32 devices in a mesh: canvas: 4 (over y, x), height: 8 (over z, core).
Axes of the slice: x: 2, y: 2, z: 4, core: 2. Of those that a mesh axis runs over, the one named last changes fastest.
Arguments:
- features: bfloat16 [4, 64, 16, 512], P('canvas', 'height')
- tile_ids: int32 [4, 64], P('canvas'), may hold values from 0 to 63, as said below
- norm_gains: float32 [3, 512], replicated, may hold values from 0.5 to 1.5
- norm_shifts: float32 [3, 512], replicated, may hold values from -1.5 to 1.5
- conv_weights: bfloat16 [2, 3, 3, 512, 512], replicated, may hold values from -0.09375 to 0.09375
- conv_biases: float32 [2, 512], replicated, may hold values from -1.5 to 1.5
- qkv_weight: bfloat16 [512, 1536], replicated, may hold values from -0.25 to 0.25
- qv_bias: float32 [2, 512], replicated, may hold values from -2.5 to 2.5
- proj_weight: bfloat16 [512, 512], replicated, may hold values from -2 to 2
- proj_bias: float32 [512], replicated, may hold values from -1.5 to 1.5
- cotangent: bfloat16 [4, 64, 16, 512], P('canvas', 'height'), may hold values from -6 to 6
Outputs:
- output: bfloat16 [4, 64, 16, 512], P('canvas', 'height')
- input_grad: bfloat16 [4, 64, 16, 512], P('canvas', 'height')
- norm_gains_grad: float32 [3, 512], replicated
- norm_shifts_grad: float32 [3, 512], replicated
- conv_weights_grad: float32 [2, 3, 3, 512, 512], P(None, None, None, 'canvas', 'height')
- conv_biases_grad: float32 [2, 512], replicated
- qkv_weight_grad: float32 [512, 1536], replicated
- qv_bias_grad: float32 [2, 512], replicated
- proj_weight_grad: float32 [512, 512], replicated
- proj_bias_grad: float32 [512], replicated
The draws below stay inside these ranges and needn't reach their ends.
Inputs may be any that keep to these rules, and one draw needn't show every extreme that they name: `tile_ids`: within each canvas a row's id is the index of the first row of its latent image, so ids start at 0 and never fall; rows that share an id form one latent image of 16 columns. One canvas holds a single image over all its rows; in every other canvas the last row begins an image of its own.
All inputs are finite; a program needn't handle non-finite values.
Results may differ from the reference program's by a relative error of at most 0.014.
Values may be sent and summed in bfloat16 or wider, within the bound.
No kernel may reach another device: no remote copies, remote signals or barrier semaphores. Data moves between devices by JAX's collectives and lax.ppermute only.
A program may use at most 256 MiB of HBM per device.

```python
import jax
import jax.numpy as jnp
from jax import lax

C = 512
GROUPS = 32
COLS = 16
ROWS = 64
CANVASES = 4


def draw_features(key, part):
    key = jax.random.fold_in(key, 11)
    key_base, key_rough, key_channel = jax.random.split(key, 3)
    shape = (CANVASES, ROWS, COLS, C)
    base = jax.random.normal(key_base, shape, jnp.float32)
    rising = 1.0 + 2.0 * jnp.arange(ROWS, dtype=jnp.float32) / (ROWS - 1)
    rough = jnp.exp(jax.random.uniform(key_rough, (CANVASES, ROWS, 1, 1), jnp.float32, -0.35, 0.35))
    channel = jnp.exp(jax.random.uniform(key_channel, (1, 1, 1, C), jnp.float32, -1.15, 1.15))
    return (base * rising[None, :, None, None] * rough * channel).astype(jnp.bfloat16)


def draw_tile_ids(key, part):
    key = jax.random.fold_in(key, 23)
    key_starts, key_whole = jax.random.split(key)
    starts = (jax.random.randint(key_starts, (CANVASES, ROWS), 0, 16) == 0).astype(jnp.int32)
    starts = starts.at[:, ROWS - 1].set(1)
    whole = jax.random.randint(key_whole, (), 0, CANVASES)
    keeping = (jnp.arange(CANVASES) != whole).astype(jnp.int32)
    row_index = jnp.arange(ROWS, dtype=jnp.int32)
    marks = starts * keeping[:, None] * row_index[None, :]
    return lax.cummax(marks, axis=1).astype(jnp.int32)


def steps_of(rng, extent, shards, smallest, largest):
    level, own = 1.0, jax.random.fold_in(rng, 6)
    for dim, shards_of in shards:
        heights = jnp.exp(jax.random.uniform(jax.random.fold_in(own, dim), (shards_of,), jnp.float32, smallest / len(shards), largest / len(shards)))
        level = level * jnp.repeat(heights, extent[dim] // shards_of).reshape([-1 if axis == dim else 1 for axis in range(len(extent))])
    return level


def noise(own_key, extent, deviation, bound, pieces=(), kind=jnp.bfloat16):
    loudness = steps_of(own_key, extent, pieces, -0.22, 0.18) if pieces else 1.0
    values = jax.random.normal(own_key, extent, jnp.float32) * deviation * loudness
    return jnp.minimum(jnp.maximum(values, -bound), bound).astype(kind)


def setup_inputs(seed: int = 0) -> dict:
    key_list = jax.random.split(jax.random.key(seed), 12)
    return {
        "features": draw_features(jax.random.fold_in(key_list[11], 71), 0),
        "tile_ids": draw_tile_ids(jax.random.fold_in(key_list[11], 71), 0),
        "norm_gains": jnp.clip(jax.random.uniform(key_list[2], (3, C), jnp.float32, 0.5, 1.5), 0.5, 1.5),
        "norm_shifts": noise(key_list[3], (3, C), 0.3, 1.5, (), jnp.float32),
        "conv_weights": noise(key_list[4], (2, 3, 3, C, C), (9 * C) ** -0.5, 0.09375),
        "conv_biases": noise(key_list[5], (2, C), 0.3, 1.5, (), jnp.float32),
        "qkv_weight": noise(key_list[6], (C, 3 * C), C ** -0.5, 0.25),
        "qv_bias": noise(key_list[7], (2, C), 0.5, 2.5, (), jnp.float32),
        "proj_weight": noise(key_list[8], (C, C), (C // 64) ** -0.5, 2.0),
        "proj_bias": noise(key_list[9], (C,), 0.3, 1.5, (), jnp.float32),
        "cotangent": noise(key_list[10], (CANVASES, ROWS, COLS, C), 1.0, 6.0, ((0, 4), (1, 8))),
    }


epsilon = 1e-06
masked_score = -1e+30
highest = lax.Precision.HIGHEST

@jax.custom_vjp
def low(v):
    return lax.optimization_barrier(v.astype(jnp.bfloat16)).astype(jnp.float32)

@jax.custom_vjp
def low_back(v):
    return v

def low_keep(v):
    return (low(v), None)

def low_pass(kept, grad):
    return (grad,)

def back_keep(v):
    return (v, None)

def back_low(kept, grad):
    return (low(grad),)
low.defvjp(low_keep, low_pass)
low_back.defvjp(back_keep, back_low)

def group_norm(values, gain, shift):
    pixels = values.shape[0]
    grouped = values.reshape(pixels, GROUPS, C // GROUPS)
    center = lax.optimization_barrier(jnp.mean(grouped, axis=(0, 2), keepdims=True))
    spread = lax.optimization_barrier(jnp.mean((grouped - center) * (grouped - center), axis=(0, 2), keepdims=True))
    normed = (grouped - center) * lax.rsqrt(spread + epsilon)
    return normed.reshape(pixels, C) * gain + shift

def swish(values):
    return values * jax.nn.sigmoid(values)

def convolve(acts, row_mask, weight, bias):
    padded = jnp.pad(acts.reshape(ROWS, COLS, C), ((1, 1), (1, 1), (0, 0)))
    total = jnp.zeros((ROWS, COLS, C), jnp.float32) + bias
    for row_tap in range(3):
        shifted = padded[row_tap:row_tap + ROWS] * row_mask[:, row_tap, None, None]
        for col_tap in range(3):
            total = total + jnp.einsum('rcd,de->rce', shifted[:, col_tap:col_tap + COLS], weight[row_tap, col_tap], precision=highest)
    return total.reshape(ROWS * COLS, C)

def attention(normed, pixel_ids, qkv_weight, qv_bias):
    mixed = jnp.dot(normed, qkv_weight, precision=highest)
    queries = low(low_back(mixed[:, :C] + qv_bias[0]))
    key_rows = low(low_back(mixed[:, C:2 * C]))
    value_rows = low(low_back(mixed[:, 2 * C:] + qv_bias[1]))
    block_rows = min(2048, ROWS * COLS)
    count_blocks = ROWS * COLS // block_rows

    def one_block(pair):
        query_block, id_block = pair
        scores = low_back(jnp.dot(query_block, key_rows.T, precision=highest) * C ** (-0.5))
        scores = jnp.where(id_block[:, None] == pixel_ids[None, :], scores, masked_score)
        weights = jax.nn.softmax(scores, axis=1)
        return jnp.dot(low(weights), value_rows, precision=highest)
    blocks = lax.map(jax.checkpoint(one_block), (queries.reshape(count_blocks, block_rows, C), pixel_ids.reshape(count_blocks, block_rows)))
    return low(low_back(blocks.reshape(ROWS * COLS, C)))

def canvas_layer(inputs, row_ids, weights):
    norm_gains, norm_shifts, conv_weights, conv_biases, qkv_weight, qv_bias, proj_weight, proj_bias = weights
    edge_ids = jnp.full((1,), -1, jnp.int32)
    padded_ids = jnp.concatenate([edge_ids, row_ids.astype(jnp.int32), edge_ids])
    row_mask = jnp.stack([padded_ids[row_tap:row_tap + ROWS] == row_ids.astype(jnp.int32) for row_tap in range(3)], axis=1).astype(jnp.float32)
    pixel_ids = jnp.repeat(row_ids.astype(jnp.int32), COLS)
    flat_input = inputs.reshape(ROWS * COLS, C)
    first_act = low(swish(group_norm(flat_input, norm_gains[0], norm_shifts[0])))
    middle = low_back(convolve(first_act, row_mask, conv_weights[0], conv_biases[0]))
    second_act = low(swish(group_norm(middle, norm_gains[1], norm_shifts[1])))
    branch = low_back(convolve(second_act, row_mask, conv_weights[1], conv_biases[1]))
    residual = flat_input + branch
    normed = low(group_norm(residual, norm_gains[2], norm_shifts[2]))
    attended = attention(normed, pixel_ids, qkv_weight, qv_bias)
    result = residual + jnp.dot(attended, proj_weight, precision=highest) + proj_bias
    return result.reshape(ROWS, COLS, C)

def reference(features, tile_ids, norm_gains, norm_shifts, conv_weights, conv_biases, qkv_weight, qv_bias, proj_weight, proj_bias, cotangent):
    parameters = (norm_gains, norm_shifts, conv_weights.astype(jnp.float32), conv_biases, qkv_weight.astype(jnp.float32), qv_bias, proj_weight.astype(jnp.float32), proj_bias)

    def forward(inputs, weights):

        def per_canvas(pair):
            return canvas_layer(pair[0], pair[1], weights)
        return lax.map(per_canvas, (inputs, tile_ids))
    result, pullback = jax.vjp(forward, features.astype(jnp.float32), parameters)
    input_grad, gradients = pullback(cotangent.astype(jnp.float32))
    return (result.astype(jnp.bfloat16), input_grad.astype(jnp.bfloat16), gradients[0], gradients[1], gradients[2], gradients[3], gradients[4], gradients[5], gradients[6], gradients[7])
```

```python
import jax
import jax.numpy as jnp
from jax import lax
from jax.sharding import PartitionSpec as P

GROUPS = 32


epsilon = 1e-06
masked_score = -1e30
MOST_PIXELS = 2048


def extended(block, sides, width):
    for axis, dim in sides:
        count = lax.axis_size(axis)
        forward = [(i, i + 1) for i in range(count - 1)]
        backward = [(target, source) for source, target in forward]
        low = lax.ppermute(
            lax.slice_in_dim(block, block.shape[dim] - width, None, axis=dim), axis, forward
        )
        high = lax.ppermute(lax.slice_in_dim(block, 0, width, axis=dim), axis, backward)
        block = jnp.concatenate([low, block, high], axis=dim)
    return block


def group_total(vector):
    return vector.reshape(GROUPS, -1).sum(axis=1)


def spread_groups(vector, channels):
    return jnp.repeat(vector, channels // GROUPS)


def norm_forward(values, gain, shift, members):
    channels = values.shape[1]
    totals = lax.psum(group_total(jnp.sum(values, axis=0)), "height")
    centered = values - spread_groups(totals / members, channels)
    squares = lax.psum(group_total(jnp.sum(centered * centered, axis=0)), "height")
    inverse = spread_groups(lax.rsqrt(squares / members + epsilon), channels)
    normed = centered * inverse
    return (normed, inverse, normed * gain + shift)


def norm_backward(grad_in, normed, inverse, gain, members):
    channels = grad_in.shape[1]
    scaled = grad_in * gain
    both_sums = lax.psum(
        (group_total(jnp.sum(scaled, axis=0)), group_total(jnp.sum(scaled * normed, axis=0))),
        "height",
    )
    mean_grad = spread_groups(both_sums[0] / members, channels)
    mean_cross = spread_groups(both_sums[1] / members, channels)
    result = inverse * (scaled - mean_grad - normed * mean_cross)
    return (result, jnp.sum(grad_in * normed, axis=0), jnp.sum(grad_in, axis=0))


def swish(values):
    return values * jax.nn.sigmoid(values)


def swish_slope(values):
    sigmoid_part = jax.nn.sigmoid(values)
    return sigmoid_part * (1.0 + values * (1.0 - sigmoid_part))


def tap_columns(padded, row_mask, local_rows, canvas_cols):
    pieces = []
    for row_tap in range(3):
        rows_taken = padded[row_tap : row_tap + local_rows] * row_mask[:, row_tap, None, None]
        for col_tap in range(3):
            pieces.append(rows_taken[:, col_tap : col_tap + canvas_cols])
    stacked = jnp.concatenate(pieces, axis=2)
    return stacked.reshape(local_rows * canvas_cols, stacked.shape[2])


def conv_forward(acts, row_mask, weight, bias):
    local_rows, canvas_cols, channels = acts.shape
    rimmed = extended(acts, (("height", 0),), 1)
    padded = jnp.pad(rimmed, ((0, 0), (1, 1), (0, 0)))
    gathered = tap_columns(padded, row_mask, local_rows, canvas_cols)
    result = (
        jnp.dot(
            gathered, weight.reshape(9 * channels, channels), preferred_element_type=jnp.float32
        )
        + bias
    )
    return (result, gathered)


def conv_backward(grad_low, row_mask, weight, gathered):
    local_rows, canvas_cols, channels = grad_low.shape
    flat_grad = grad_low.reshape(local_rows * canvas_cols, channels)
    weight_grad = lax.dot_general(
        gathered, flat_grad, (((0,), (0,)), ((), ())), preferred_element_type=jnp.float32
    )
    rimmed = extended(grad_low, (("height", 0),), 1)
    padded = jnp.pad(rimmed, ((0, 0), (1, 1), (0, 0)))
    grad_taps = tap_columns(padded, row_mask, local_rows, canvas_cols)
    flipped = jnp.transpose(weight[::-1, ::-1], (0, 1, 3, 2)).reshape(9 * channels, channels)
    input_part = jnp.dot(grad_taps, flipped, preferred_element_type=jnp.float32)
    return (
        input_part,
        weight_grad.reshape(3, 3, channels, channels),
        jnp.sum(flat_grad.astype(jnp.float32), axis=0),
    )


def take_rows(array, offset, count):
    return lax.dynamic_slice_in_dim(array, offset, count)


def score_grads(
    queries, out_grad, log_total, row_dots, query_ids, key_rows, value_rows, key_ids, score_scale
):
    scores = (
        lax.dot_general(
            queries, key_rows, (((1,), (1,)), ((), ())), preferred_element_type=jnp.float32
        )
        * score_scale
    )
    same_tile = query_ids[:, None] == key_ids[None, :]
    softmax_block = jnp.exp(jnp.where(same_tile, scores - log_total[:, None], masked_score))
    weight_grad = lax.dot_general(
        out_grad, value_rows, (((1,), (1,)), ((), ())), preferred_element_type=jnp.float32
    )
    score_grad = (softmax_block * (weight_grad - row_dots[:, None])).astype(jnp.bfloat16)
    return (softmax_block.astype(jnp.bfloat16), score_grad)


def split_canvas(
    features,
    tile_ids,
    norm_gains,
    norm_shifts,
    conv_weights,
    conv_biases,
    qkv_weight,
    qv_bias,
    proj_weight,
    proj_bias,
    cotangent,
):
    height_size = lax.axis_size("height")
    local_rows = features.shape[1]
    canvas_cols = features.shape[2]
    channels = features.shape[3]
    pixels = local_rows * canvas_cols
    row_ids = tile_ids[0]
    all_rows = row_ids.shape[0]
    members = float(all_rows * canvas_cols * (channels // GROUPS))
    score_scale = channels ** (-0.5)
    first_row = lax.axis_index("height") * local_rows
    edge_ids = jnp.full((1,), -1, jnp.int32)
    padded_ids = jnp.concatenate([edge_ids, row_ids, edge_ids])
    near_ids = lax.dynamic_slice_in_dim(padded_ids, first_row, local_rows + 2)
    own_rows = near_ids[1 : local_rows + 1]
    row_mask = jnp.stack(
        [near_ids[row_tap : row_tap + local_rows] == own_rows for row_tap in range(3)], axis=1
    ).astype(jnp.bfloat16)
    key_ids = jnp.repeat(row_ids, canvas_cols)
    query_ids = jnp.repeat(own_rows, canvas_cols)
    grid_shape = (local_rows, canvas_cols, channels)
    inputs = features[0].reshape(pixels, channels).astype(jnp.float32)
    normed_one, inverse_one, pre_one = norm_forward(inputs, norm_gains[0], norm_shifts[0], members)
    act_one = swish(pre_one).astype(jnp.bfloat16).reshape(grid_shape)
    middle, taps_one = conv_forward(act_one, row_mask, conv_weights[0], conv_biases[0])
    normed_two, inverse_two, pre_two = norm_forward(middle, norm_gains[1], norm_shifts[1], members)
    act_two = swish(pre_two).astype(jnp.bfloat16).reshape(grid_shape)
    branch, taps_two = conv_forward(act_two, row_mask, conv_weights[1], conv_biases[1])
    residual = inputs + branch
    normed_three, inverse_three, pre_three = norm_forward(
        residual, norm_gains[2], norm_shifts[2], members
    )
    attn_input = pre_three.astype(jnp.bfloat16)
    mixed = jnp.dot(attn_input, qkv_weight, preferred_element_type=jnp.float32)
    queries = (mixed[:, :channels] + qv_bias[0]).astype(jnp.bfloat16)
    key_rows = mixed[:, channels : 2 * channels].astype(jnp.bfloat16)
    value_rows = (mixed[:, 2 * channels :] + qv_bias[1]).astype(jnp.bfloat16)
    running_max = jnp.full((pixels,), masked_score, jnp.float32)
    key_piece = lax.all_gather(key_rows, "height", axis=0, tiled=True)
    value_piece = lax.all_gather(value_rows, "height", axis=0, tiled=True)
    scores = (
        lax.dot_general(
            queries, key_piece, (((1,), (1,)), ((), ())), preferred_element_type=jnp.float32
        )
        * score_scale
    )
    same_tile = query_ids[:, None] == key_ids[None, :]
    scores = jnp.where(same_tile, scores, masked_score)
    new_max = jnp.maximum(running_max, jnp.max(scores, axis=1))
    weights = jnp.where(same_tile, jnp.exp(scores - new_max[:, None]), 0.0)
    summed_out = jnp.dot(
        weights.astype(jnp.bfloat16), value_piece, preferred_element_type=jnp.float32
    )
    total_weight = jnp.sum(weights, axis=1)
    log_total = new_max + jnp.log(total_weight)
    attended = summed_out / total_weight[:, None]
    attended_low = attended.astype(jnp.bfloat16)
    output = (
        residual
        + jnp.dot(attended_low, proj_weight, preferred_element_type=jnp.float32)
        + proj_bias
    )
    out_grad = cotangent[0].reshape(pixels, channels)
    out_grad_full = out_grad.astype(jnp.float32)
    proj_grad = lax.dot_general(
        attended_low, out_grad, (((0,), (0,)), ((), ())), preferred_element_type=jnp.float32
    )
    proj_bias_grad = jnp.sum(out_grad_full, axis=0)
    attended_grad = lax.dot_general(
        out_grad, proj_weight, (((1,), (1,)), ((), ())), preferred_element_type=jnp.float32
    ).astype(jnp.bfloat16)
    row_dots = jnp.sum(attended_grad.astype(jnp.float32) * attended, axis=1)
    block_rows = pixels * min(height_size, 8)
    zero_block = jnp.zeros((pixels, channels), jnp.float32)
    key_all, value_all = (
        lax.all_gather(key_rows, "height", axis=0, tiled=True),
        lax.all_gather(value_rows, "height", axis=0, tiled=True),
    )
    query_all, grad_all = (
        lax.all_gather(queries, "height", axis=0, tiled=True),
        lax.all_gather(attended_grad, "height", axis=0, tiled=True),
    )
    total_all, dots_all = (
        lax.all_gather(log_total, "height", axis=0, tiled=True),
        lax.all_gather(row_dots, "height", axis=0, tiled=True),
    )

    def own_query_step(running, block_index):
        offset = block_index * block_rows
        key_part = take_rows(key_all, offset, block_rows)
        rounded, score_grad = score_grads(
            queries,
            attended_grad,
            log_total,
            row_dots,
            query_ids,
            key_part,
            take_rows(value_all, offset, block_rows),
            take_rows(key_ids, offset, block_rows),
            score_scale,
        )
        return (
            running
            + jnp.dot(score_grad, key_part, preferred_element_type=jnp.float32) * score_scale,
            None,
        )

    def own_key_step(running, block_index):
        offset = block_index * block_rows
        query_part = take_rows(query_all, offset, block_rows)
        grad_part = take_rows(grad_all, offset, block_rows)
        rounded, score_grad = score_grads(
            query_part,
            grad_part,
            take_rows(total_all, offset, block_rows),
            take_rows(dots_all, offset, block_rows),
            take_rows(key_ids, offset, block_rows),
            key_rows,
            value_rows,
            query_ids,
            score_scale,
        )
        key_part = (
            lax.dot_general(
                score_grad, query_part, (((0,), (0,)), ((), ())), preferred_element_type=jnp.float32
            )
            * score_scale
        )
        value_part = lax.dot_general(
            rounded, grad_part, (((0,), (0,)), ((), ())), preferred_element_type=jnp.float32
        )
        return ((running[0] + key_part, running[1] + value_part), None)

    block_count = key_all.shape[0] // block_rows
    query_grad, unused_one = lax.scan(own_query_step, zero_block, jnp.arange(block_count))
    (key_grad, value_grad), unused_two = lax.scan(
        own_key_step, (zero_block, zero_block), jnp.arange(block_count)
    )
    query_low = query_grad.astype(jnp.bfloat16)
    key_low = key_grad.astype(jnp.bfloat16)
    value_low = value_grad.astype(jnp.bfloat16)
    stacked_grad = jnp.concatenate([query_low, key_low, value_low], axis=1)
    qkv_grad = lax.dot_general(
        attn_input, stacked_grad, (((0,), (0,)), ((), ())), preferred_element_type=jnp.float32
    )
    qv_grad = jnp.stack(
        [
            jnp.sum(query_low.astype(jnp.float32), axis=0),
            jnp.sum(value_low.astype(jnp.float32), axis=0),
        ]
    )
    normed_grad = lax.dot_general(
        stacked_grad, qkv_weight, (((1,), (1,)), ((), ())), preferred_element_type=jnp.float32
    )
    back_three, gain_three, shift_three = norm_backward(
        normed_grad, normed_three, inverse_three, norm_gains[2], members
    )
    residual_grad = out_grad_full + back_three
    grad_two = residual_grad.astype(jnp.bfloat16).reshape(grid_shape)
    act_two_grad, weight_two_grad, bias_two_grad = conv_backward(
        grad_two, row_mask, conv_weights[1], taps_two
    )
    middle_grad, gain_two, shift_two = norm_backward(
        act_two_grad * swish_slope(pre_two), normed_two, inverse_two, norm_gains[1], members
    )
    grad_one = middle_grad.astype(jnp.bfloat16).reshape(grid_shape)
    act_one_grad, weight_one_grad, bias_one_grad = conv_backward(
        grad_one, row_mask, conv_weights[0], taps_one
    )
    input_back, gain_one, shift_one = norm_backward(
        act_one_grad * swish_slope(pre_one), normed_one, inverse_one, norm_gains[0], members
    )
    input_grad = residual_grad + input_back
    conv_grad = jnp.stack([weight_one_grad, weight_two_grad])
    conv_part = lax.psum_scatter(conv_grad, "height", scatter_dimension=4, tiled=True)
    conv_part = lax.psum_scatter(
        conv_part.astype(jnp.bfloat16), "canvas", scatter_dimension=3, tiled=True
    ).astype(jnp.float32)
    summed = lax.psum(
        (
            jnp.stack([gain_one, gain_two, gain_three]),
            jnp.stack([shift_one, shift_two, shift_three]),
            jnp.stack([bias_one_grad, bias_two_grad]),
            qkv_grad,
            qv_grad,
            proj_grad,
            proj_bias_grad,
        ),
        ("canvas", "height"),
    )
    return (
        output.astype(jnp.bfloat16).reshape((1,) + grid_shape),
        input_grad.astype(jnp.bfloat16).reshape((1,) + grid_shape),
        summed[0],
        summed[1],
        conv_part,
        summed[2],
        summed[3],
        summed[4],
        summed[5],
        summed[6],
    )


def whole_canvas(
    features,
    tile_ids,
    norm_gains,
    norm_shifts,
    conv_weights,
    conv_biases,
    qkv_weight,
    qv_bias,
    proj_weight,
    proj_bias,
    cotangent,
):
    height_size = lax.axis_size("height")
    canvas_size = lax.axis_size("canvas")
    local_rows, canvas_cols, channels = features.shape[1:]
    row_ids = tile_ids[0]
    all_rows = row_ids.shape[0]
    pixels = all_rows * canvas_cols
    own_pixels = local_rows * canvas_cols
    members = float(pixels * (channels // GROUPS))
    score_scale = channels ** (-0.5)
    height_index = lax.axis_index("height")
    grid_shape = (all_rows, canvas_cols, channels)
    edge_ids = jnp.full((1,), -1, jnp.int32)
    padded_ids = jnp.concatenate([edge_ids, row_ids, edge_ids])
    row_mask = jnp.stack(
        [padded_ids[row_tap : row_tap + all_rows] == row_ids for row_tap in range(3)], axis=1
    ).astype(jnp.bfloat16)
    pixel_ids = jnp.repeat(row_ids, canvas_cols)
    same_tile = pixel_ids[:, None] == pixel_ids[None, :]

    all_features = lax.all_gather(features[0], "height", axis=0, tiled=True)
    late_cotangent, all_features = lax.optimization_barrier((cotangent[0], all_features))
    out_grad = lax.all_gather(late_cotangent, "height", axis=0, tiled=True).reshape(pixels, channels)

    def norm(values, which):
        totals = group_total(jnp.sum(values, axis=0))
        centered = values - spread_groups(totals / members, channels)
        squares = group_total(jnp.sum(centered * centered, axis=0))
        inverse = spread_groups(lax.rsqrt(squares / members + epsilon), channels)
        normed = centered * inverse
        return normed, inverse, normed * norm_gains[which] + norm_shifts[which]

    def norm_back(grad_in, normed, inverse, which):
        scaled = grad_in * norm_gains[which]
        mean_grad = spread_groups(group_total(jnp.sum(scaled, axis=0)) / members, channels)
        mean_cross = spread_groups(group_total(jnp.sum(scaled * normed, axis=0)) / members, channels)
        result = inverse * (scaled - mean_grad - normed * mean_cross)
        return result, jnp.sum(grad_in * normed, axis=0), jnp.sum(grad_in, axis=0)

    def taps(block):
        padded = jnp.pad(block.reshape(grid_shape), ((1, 1), (1, 1), (0, 0)))
        return tap_columns(padded, row_mask, all_rows, canvas_cols)

    def conv(acts, which):
        return (
            jnp.dot(
                taps(acts),
                conv_weights[which].reshape(9 * channels, channels),
                preferred_element_type=jnp.float32,
            )
            + conv_biases[which]
        )

    def conv_back(grad_low, which):
        flipped = jnp.transpose(conv_weights[which, ::-1, ::-1], (0, 1, 3, 2))
        return jnp.dot(
            taps(grad_low),
            flipped.reshape(9 * channels, channels),
            preferred_element_type=jnp.float32,
        )

    out_share = channels // height_size

    def conv_weight_part(acts, grad_low):
        own = lax.dynamic_slice_in_dim(grad_low, height_index * out_share, out_share, axis=1)
        padded = jnp.pad(own.reshape(all_rows, canvas_cols, out_share), ((1, 1), (1, 1), (0, 0)))
        pieces = []
        for row_tap in range(3):
            rows_taken = padded[2 - row_tap : 2 - row_tap + all_rows] * row_mask[:, 2 - row_tap, None, None]
            for col_tap in range(3):
                pieces.append(rows_taken[:, 2 - col_tap : 2 - col_tap + canvas_cols])
        stacked = jnp.concatenate(pieces, axis=2).reshape(pixels, 9 * out_share)
        return lax.dot_general(
            acts, stacked, (((0,), (0,)), ((), ())), preferred_element_type=jnp.float32
        )

    def canvas_total(part):
        canvas_index = lax.axis_index("canvas")
        share = part.shape[0] // canvas_size
        total = lax.dynamic_slice_in_dim(part, canvas_index * share, share)
        for step in range(1, canvas_size):
            pairs = [(i, i ^ step if canvas_size & (canvas_size - 1) == 0 else (i + step) % canvas_size) for i in range(canvas_size)]
            target = jnp.asarray([t for _, t in pairs])[canvas_index]
            sent = lax.dynamic_slice_in_dim(part, target * share, share).astype(jnp.bfloat16)
            total = total + lax.ppermute(sent, "canvas", pairs).astype(jnp.float32)
        return total

    inputs = all_features.reshape(pixels, channels).astype(jnp.float32)
    normed_one, inverse_one, pre_one = norm(inputs, 0)
    act_one = swish(pre_one).astype(jnp.bfloat16)
    middle = conv(act_one, 0)
    normed_two, inverse_two, pre_two = norm(middle, 1)
    act_two = swish(pre_two).astype(jnp.bfloat16)
    residual = inputs + conv(act_two, 1)
    normed_three, inverse_three, pre_three = norm(residual, 2)
    attn_input = pre_three.astype(jnp.bfloat16)
    mixed = jnp.dot(attn_input, qkv_weight, preferred_element_type=jnp.float32)
    queries = (mixed[:, :channels] + qv_bias[0]).astype(jnp.bfloat16)
    key_rows = mixed[:, channels : 2 * channels].astype(jnp.bfloat16)
    value_rows = (mixed[:, 2 * channels :] + qv_bias[1]).astype(jnp.bfloat16)
    scores = (
        lax.dot_general(
            queries, key_rows, (((1,), (1,)), ((), ())), preferred_element_type=jnp.float32
        )
        * score_scale
    )
    scores = jnp.where(same_tile, scores, masked_score)
    weights = jnp.exp(scores - jnp.max(scores, axis=1, keepdims=True))
    weights = weights / jnp.sum(weights, axis=1, keepdims=True)
    rounded = weights.astype(jnp.bfloat16)
    attended = jnp.dot(rounded, value_rows, preferred_element_type=jnp.float32).astype(jnp.bfloat16)
    own_attended = lax.dynamic_slice_in_dim(attended, height_index * own_pixels, own_pixels)
    own_residual = lax.dynamic_slice_in_dim(residual, height_index * own_pixels, own_pixels)
    output = (
        own_residual
        + jnp.dot(own_attended, proj_weight, preferred_element_type=jnp.float32)
        + proj_bias
    )
    attended_grad = lax.dot_general(
        out_grad, proj_weight, (((1,), (1,)), ((), ())), preferred_element_type=jnp.float32
    ).astype(jnp.bfloat16)
    weight_grad = lax.dot_general(
        attended_grad, value_rows, (((1,), (1,)), ((), ())), preferred_element_type=jnp.float32
    )
    row_dots = jnp.sum(weights * weight_grad, axis=1, keepdims=True)
    score_grad = (weights * (weight_grad - row_dots)).astype(jnp.bfloat16)
    query_low = (
        jnp.dot(score_grad, key_rows, preferred_element_type=jnp.float32) * score_scale
    ).astype(jnp.bfloat16)
    key_low = (
        lax.dot_general(
            score_grad, queries, (((0,), (0,)), ((), ())), preferred_element_type=jnp.float32
        )
        * score_scale
    ).astype(jnp.bfloat16)
    value_low = lax.dot_general(
        rounded, attended_grad, (((0,), (0,)), ((), ())), preferred_element_type=jnp.float32
    ).astype(jnp.bfloat16)
    stacked_grad = jnp.concatenate([query_low, key_low, value_low], axis=1)
    row_share = channels // height_size
    own_input = lax.dynamic_slice_in_dim(attn_input, height_index * row_share, row_share, axis=1)
    own_out = lax.dynamic_slice_in_dim(attended, height_index * row_share, row_share, axis=1)
    qkv_part = lax.dot_general(
        own_input, stacked_grad, (((0,), (0,)), ((), ())), preferred_element_type=jnp.float32
    )
    proj_part = lax.dot_general(
        own_out, out_grad, (((0,), (0,)), ((), ())), preferred_element_type=jnp.float32
    )
    mixed_part = canvas_total(jnp.concatenate([qkv_part, proj_part], axis=1))
    mixed_grad = lax.all_gather(
        mixed_part.astype(jnp.bfloat16), ("height", "canvas"), axis=0, tiled=True
    )
    qkv_grad = mixed_grad[:, : 3 * channels].astype(jnp.float32)
    proj_grad = mixed_grad[:, 3 * channels :].astype(jnp.float32)

    normed_grad = lax.dot_general(
        stacked_grad, qkv_weight, (((1,), (1,)), ((), ())), preferred_element_type=jnp.float32
    )
    back_three, gain_three, shift_three = norm_back(normed_grad, normed_three, inverse_three, 2)
    residual_grad = out_grad.astype(jnp.float32) + back_three
    grad_two = residual_grad.astype(jnp.bfloat16)
    conv_two = canvas_total(conv_weight_part(act_two, grad_two))
    act_two_grad = conv_back(grad_two, 1)
    middle_grad, gain_two, shift_two = norm_back(
        act_two_grad * swish_slope(pre_two), normed_two, inverse_two, 1
    )
    grad_one = middle_grad.astype(jnp.bfloat16)
    conv_one = canvas_total(conv_weight_part(act_one, grad_one))
    act_one_grad = conv_back(grad_one, 0)
    input_back, gain_one, shift_one = norm_back(
        act_one_grad * swish_slope(pre_one), normed_one, inverse_one, 0
    )
    input_grad = lax.dynamic_slice_in_dim(
        residual_grad + input_back, height_index * own_pixels, own_pixels
    )
    wide = jnp.float32
    vectors = jnp.stack(
        [
            gain_one,
            gain_two,
            gain_three,
            shift_one,
            shift_two,
            shift_three,
            jnp.sum(grad_one.astype(wide), axis=0),
            jnp.sum(grad_two.astype(wide), axis=0),
            jnp.sum(query_low.astype(wide), axis=0),
            jnp.sum(value_low.astype(wide), axis=0),
            jnp.sum(out_grad.astype(wide), axis=0),
        ]
    )
    vectors = lax.psum(vectors, "canvas")
    conv_grad = jnp.stack([conv_one, conv_two]).reshape(
        2, channels // canvas_size, 3, 3, out_share
    )
    own_shape = (1, local_rows, canvas_cols, channels)
    return (
        output.astype(jnp.bfloat16).reshape(own_shape),
        input_grad.astype(jnp.bfloat16).reshape(own_shape),
        vectors[0:3],
        vectors[3:6],
        jnp.transpose(conv_grad, (0, 2, 3, 1, 4)),
        vectors[6:8],
        qkv_grad,
        vectors[8:10],
        proj_grad,
        vectors[10],
    )


def on_device(*arrays):
    canvas_pixels = arrays[1].shape[1] * arrays[0].shape[2]
    plan = whole_canvas if canvas_pixels <= MOST_PIXELS else split_canvas
    return plan(*arrays)


def solution(mesh):
    in_specs = (
        P("canvas", "height", None, None),
        P("canvas", None),
        P(),
        P(),
        P(),
        P(),
        P(),
        P(),
        P(),
        P(),
        P("canvas", "height", None, None),
    )
    out_specs = (
        P("canvas", "height", None, None),
        P("canvas", "height", None, None),
        P(),
        P(),
        P(None, None, None, "canvas", "height"),
        P(),
        P(),
        P(),
        P(),
        P(),
    )
    return jax.shard_map(
        on_device, mesh=mesh, in_specs=in_specs, out_specs=out_specs, check_vma=False
    )
```

```python
import functools

import jax
import jax.numpy as jnp
from jax import lax
from jax.experimental import pallas as pl
from jax.experimental.pallas import tpu as pltpu
from jax.sharding import PartitionSpec as P

GROUPS = 32


epsilon = 1e-06
masked_score = -1e30
MOST_PIXELS = 1024
LANES = 128
NARROW = 128
CHUNK = 128
CONV_ROWS = 512
QUERY_ROWS = 256
VMEM_BYTES = 48 * 2**20


def extended(block, sides, width):
    for axis, dim in sides:
        count = lax.axis_size(axis)
        forward = [(i, i + 1) for i in range(count - 1)]
        backward = [(target, source) for source, target in forward]
        low = lax.ppermute(
            lax.slice_in_dim(block, block.shape[dim] - width, None, axis=dim), axis, forward
        )
        high = lax.ppermute(lax.slice_in_dim(block, 0, width, axis=dim), axis, backward)
        block = jnp.concatenate([low, block, high], axis=dim)
    return block


def group_total(vector):
    return vector.reshape(GROUPS, -1).sum(axis=1)


def spread_groups(vector, channels):
    return jnp.repeat(vector, channels // GROUPS)


def norm_forward(values, gain, shift, members):
    channels = values.shape[1]
    totals = lax.psum(group_total(jnp.sum(values, axis=0)), "height")
    centered = values - spread_groups(totals / members, channels)
    squares = lax.psum(group_total(jnp.sum(centered * centered, axis=0)), "height")
    inverse = spread_groups(lax.rsqrt(squares / members + epsilon), channels)
    normed = centered * inverse
    return (normed, inverse, normed * gain + shift)


def norm_backward(grad_in, normed, inverse, gain, members):
    channels = grad_in.shape[1]
    scaled = grad_in * gain
    both_sums = lax.psum(
        (group_total(jnp.sum(scaled, axis=0)), group_total(jnp.sum(scaled * normed, axis=0))),
        "height",
    )
    mean_grad = spread_groups(both_sums[0] / members, channels)
    mean_cross = spread_groups(both_sums[1] / members, channels)
    result = inverse * (scaled - mean_grad - normed * mean_cross)
    return (result, jnp.sum(grad_in * normed, axis=0), jnp.sum(grad_in, axis=0))


def swish(values):
    return values * jax.nn.sigmoid(values)


def swish_slope(values):
    sigmoid_part = jax.nn.sigmoid(values)
    return sigmoid_part * (1.0 + values * (1.0 - sigmoid_part))


def tap_columns(padded, row_mask, local_rows, canvas_cols):
    pieces = []
    for row_tap in range(3):
        rows_taken = padded[row_tap : row_tap + local_rows] * row_mask[:, row_tap, None, None]
        for col_tap in range(3):
            pieces.append(rows_taken[:, col_tap : col_tap + canvas_cols])
    stacked = jnp.concatenate(pieces, axis=2)
    return stacked.reshape(local_rows * canvas_cols, stacked.shape[2])


def conv_forward(acts, row_mask, weight, bias):
    local_rows, canvas_cols, channels = acts.shape
    rimmed = extended(acts, (("height", 0),), 1)
    padded = jnp.pad(rimmed, ((0, 0), (1, 1), (0, 0)))
    gathered = tap_columns(padded, row_mask, local_rows, canvas_cols)
    result = (
        jnp.dot(
            gathered, weight.reshape(9 * channels, channels), preferred_element_type=jnp.float32
        )
        + bias
    )
    return (result, gathered)


def conv_backward(grad_low, row_mask, weight, gathered):
    local_rows, canvas_cols, channels = grad_low.shape
    flat_grad = grad_low.reshape(local_rows * canvas_cols, channels)
    weight_grad = lax.dot_general(
        gathered, flat_grad, (((0,), (0,)), ((), ())), preferred_element_type=jnp.float32
    )
    rimmed = extended(grad_low, (("height", 0),), 1)
    padded = jnp.pad(rimmed, ((0, 0), (1, 1), (0, 0)))
    grad_taps = tap_columns(padded, row_mask, local_rows, canvas_cols)
    flipped = jnp.transpose(weight[::-1, ::-1], (0, 1, 3, 2)).reshape(9 * channels, channels)
    input_part = jnp.dot(grad_taps, flipped, preferred_element_type=jnp.float32)
    return (
        input_part,
        weight_grad.reshape(3, 3, channels, channels),
        jnp.sum(flat_grad.astype(jnp.float32), axis=0),
    )


def take_rows(array, offset, count):
    return lax.dynamic_slice_in_dim(array, offset, count)


def score_grads(
    queries, out_grad, log_total, row_dots, query_ids, key_rows, value_rows, key_ids, score_scale
):
    scores = (
        lax.dot_general(
            queries, key_rows, (((1,), (1,)), ((), ())), preferred_element_type=jnp.float32
        )
        * score_scale
    )
    same_tile = query_ids[:, None] == key_ids[None, :]
    softmax_block = jnp.exp(jnp.where(same_tile, scores - log_total[:, None], masked_score))
    weight_grad = lax.dot_general(
        out_grad, value_rows, (((1,), (1,)), ((), ())), preferred_element_type=jnp.float32
    )
    score_grad = (softmax_block * (weight_grad - row_dots[:, None])).astype(jnp.bfloat16)
    return (softmax_block.astype(jnp.bfloat16), score_grad)


def split_canvas(
    features,
    tile_ids,
    norm_gains,
    norm_shifts,
    conv_weights,
    conv_biases,
    qkv_weight,
    qv_bias,
    proj_weight,
    proj_bias,
    cotangent,
):
    height_size = lax.axis_size("height")
    local_rows = features.shape[1]
    canvas_cols = features.shape[2]
    channels = features.shape[3]
    pixels = local_rows * canvas_cols
    row_ids = tile_ids[0]
    all_rows = row_ids.shape[0]
    members = float(all_rows * canvas_cols * (channels // GROUPS))
    score_scale = channels ** (-0.5)
    first_row = lax.axis_index("height") * local_rows
    edge_ids = jnp.full((1,), -1, jnp.int32)
    padded_ids = jnp.concatenate([edge_ids, row_ids, edge_ids])
    near_ids = lax.dynamic_slice_in_dim(padded_ids, first_row, local_rows + 2)
    own_rows = near_ids[1 : local_rows + 1]
    row_mask = jnp.stack(
        [near_ids[row_tap : row_tap + local_rows] == own_rows for row_tap in range(3)], axis=1
    ).astype(jnp.bfloat16)
    key_ids = jnp.repeat(row_ids, canvas_cols)
    query_ids = jnp.repeat(own_rows, canvas_cols)
    grid_shape = (local_rows, canvas_cols, channels)
    inputs = features[0].reshape(pixels, channels).astype(jnp.float32)
    normed_one, inverse_one, pre_one = norm_forward(inputs, norm_gains[0], norm_shifts[0], members)
    act_one = swish(pre_one).astype(jnp.bfloat16).reshape(grid_shape)
    middle, taps_one = conv_forward(act_one, row_mask, conv_weights[0], conv_biases[0])
    normed_two, inverse_two, pre_two = norm_forward(middle, norm_gains[1], norm_shifts[1], members)
    act_two = swish(pre_two).astype(jnp.bfloat16).reshape(grid_shape)
    branch, taps_two = conv_forward(act_two, row_mask, conv_weights[1], conv_biases[1])
    residual = inputs + branch
    normed_three, inverse_three, pre_three = norm_forward(
        residual, norm_gains[2], norm_shifts[2], members
    )
    attn_input = pre_three.astype(jnp.bfloat16)
    mixed = jnp.dot(attn_input, qkv_weight, preferred_element_type=jnp.float32)
    queries = (mixed[:, :channels] + qv_bias[0]).astype(jnp.bfloat16)
    key_rows = mixed[:, channels : 2 * channels].astype(jnp.bfloat16)
    value_rows = (mixed[:, 2 * channels :] + qv_bias[1]).astype(jnp.bfloat16)
    running_max = jnp.full((pixels,), masked_score, jnp.float32)
    key_piece = lax.all_gather(key_rows, "height", axis=0, tiled=True)
    value_piece = lax.all_gather(value_rows, "height", axis=0, tiled=True)
    scores = (
        lax.dot_general(
            queries, key_piece, (((1,), (1,)), ((), ())), preferred_element_type=jnp.float32
        )
        * score_scale
    )
    same_tile = query_ids[:, None] == key_ids[None, :]
    scores = jnp.where(same_tile, scores, masked_score)
    new_max = jnp.maximum(running_max, jnp.max(scores, axis=1))
    weights = jnp.where(same_tile, jnp.exp(scores - new_max[:, None]), 0.0)
    summed_out = jnp.dot(
        weights.astype(jnp.bfloat16), value_piece, preferred_element_type=jnp.float32
    )
    total_weight = jnp.sum(weights, axis=1)
    log_total = new_max + jnp.log(total_weight)
    attended = summed_out / total_weight[:, None]
    attended_low = attended.astype(jnp.bfloat16)
    output = (
        residual
        + jnp.dot(attended_low, proj_weight, preferred_element_type=jnp.float32)
        + proj_bias
    )
    out_grad = cotangent[0].reshape(pixels, channels)
    out_grad_full = out_grad.astype(jnp.float32)
    proj_grad = lax.dot_general(
        attended_low, out_grad, (((0,), (0,)), ((), ())), preferred_element_type=jnp.float32
    )
    proj_bias_grad = jnp.sum(out_grad_full, axis=0)
    attended_grad = lax.dot_general(
        out_grad, proj_weight, (((1,), (1,)), ((), ())), preferred_element_type=jnp.float32
    ).astype(jnp.bfloat16)
    row_dots = jnp.sum(attended_grad.astype(jnp.float32) * attended, axis=1)
    block_rows = pixels * min(height_size, 8)
    zero_block = jnp.zeros((pixels, channels), jnp.float32)
    key_all, value_all = (
        lax.all_gather(key_rows, "height", axis=0, tiled=True),
        lax.all_gather(value_rows, "height", axis=0, tiled=True),
    )
    query_all, grad_all = (
        lax.all_gather(queries, "height", axis=0, tiled=True),
        lax.all_gather(attended_grad, "height", axis=0, tiled=True),
    )
    total_all, dots_all = (
        lax.all_gather(log_total, "height", axis=0, tiled=True),
        lax.all_gather(row_dots, "height", axis=0, tiled=True),
    )

    def own_query_step(running, block_index):
        offset = block_index * block_rows
        key_part = take_rows(key_all, offset, block_rows)
        rounded, score_grad = score_grads(
            queries,
            attended_grad,
            log_total,
            row_dots,
            query_ids,
            key_part,
            take_rows(value_all, offset, block_rows),
            take_rows(key_ids, offset, block_rows),
            score_scale,
        )
        return (
            running
            + jnp.dot(score_grad, key_part, preferred_element_type=jnp.float32) * score_scale,
            None,
        )

    def own_key_step(running, block_index):
        offset = block_index * block_rows
        query_part = take_rows(query_all, offset, block_rows)
        grad_part = take_rows(grad_all, offset, block_rows)
        rounded, score_grad = score_grads(
            query_part,
            grad_part,
            take_rows(total_all, offset, block_rows),
            take_rows(dots_all, offset, block_rows),
            take_rows(key_ids, offset, block_rows),
            key_rows,
            value_rows,
            query_ids,
            score_scale,
        )
        key_part = (
            lax.dot_general(
                score_grad, query_part, (((0,), (0,)), ((), ())), preferred_element_type=jnp.float32
            )
            * score_scale
        )
        value_part = lax.dot_general(
            rounded, grad_part, (((0,), (0,)), ((), ())), preferred_element_type=jnp.float32
        )
        return ((running[0] + key_part, running[1] + value_part), None)

    block_count = key_all.shape[0] // block_rows
    query_grad, unused_one = lax.scan(own_query_step, zero_block, jnp.arange(block_count))
    (key_grad, value_grad), unused_two = lax.scan(
        own_key_step, (zero_block, zero_block), jnp.arange(block_count)
    )
    query_low = query_grad.astype(jnp.bfloat16)
    key_low = key_grad.astype(jnp.bfloat16)
    value_low = value_grad.astype(jnp.bfloat16)
    stacked_grad = jnp.concatenate([query_low, key_low, value_low], axis=1)
    qkv_grad = lax.dot_general(
        attn_input, stacked_grad, (((0,), (0,)), ((), ())), preferred_element_type=jnp.float32
    )
    qv_grad = jnp.stack(
        [
            jnp.sum(query_low.astype(jnp.float32), axis=0),
            jnp.sum(value_low.astype(jnp.float32), axis=0),
        ]
    )
    normed_grad = lax.dot_general(
        stacked_grad, qkv_weight, (((1,), (1,)), ((), ())), preferred_element_type=jnp.float32
    )
    back_three, gain_three, shift_three = norm_backward(
        normed_grad, normed_three, inverse_three, norm_gains[2], members
    )
    residual_grad = out_grad_full + back_three
    grad_two = residual_grad.astype(jnp.bfloat16).reshape(grid_shape)
    act_two_grad, weight_two_grad, bias_two_grad = conv_backward(
        grad_two, row_mask, conv_weights[1], taps_two
    )
    middle_grad, gain_two, shift_two = norm_backward(
        act_two_grad * swish_slope(pre_two), normed_two, inverse_two, norm_gains[1], members
    )
    grad_one = middle_grad.astype(jnp.bfloat16).reshape(grid_shape)
    act_one_grad, weight_one_grad, bias_one_grad = conv_backward(
        grad_one, row_mask, conv_weights[0], taps_one
    )
    input_back, gain_one, shift_one = norm_backward(
        act_one_grad * swish_slope(pre_one), normed_one, inverse_one, norm_gains[0], members
    )
    input_grad = residual_grad + input_back
    conv_grad = jnp.stack([weight_one_grad, weight_two_grad])
    conv_part = lax.psum_scatter(conv_grad, "height", scatter_dimension=4, tiled=True)
    conv_part = lax.psum_scatter(
        conv_part.astype(jnp.bfloat16), "canvas", scatter_dimension=3, tiled=True
    ).astype(jnp.float32)
    summed = lax.psum(
        (
            jnp.stack([gain_one, gain_two, gain_three]),
            jnp.stack([shift_one, shift_two, shift_three]),
            jnp.stack([bias_one_grad, bias_two_grad]),
            qkv_grad,
            qv_grad,
            proj_grad,
            proj_bias_grad,
        ),
        ("canvas", "height"),
    )
    return (
        output.astype(jnp.bfloat16).reshape((1,) + grid_shape),
        input_grad.astype(jnp.bfloat16).reshape((1,) + grid_shape),
        summed[0],
        summed[1],
        conv_part,
        summed[2],
        summed[3],
        summed[4],
        summed[5],
        summed[6],
    )


def fold(block):
    rows, width = block.shape
    return jnp.sum(block.reshape(rows // 8, 8, width), axis=0)


def group_lanes(block, group):
    lane = lax.broadcasted_iota(jnp.int32, block.shape, 1)
    width = block.shape[1]
    step = 1
    while step < group:
        above = pltpu.roll(block, step, 1)
        below = pltpu.roll(block, width - step, 1)
        block = block + jnp.where((lane & step) != 0, above, below)
        step *= 2
    return block


def group_mean(partial, members):
    spread = group_lanes(partial, partial.shape[1] // GROUPS)
    return jnp.sum(spread, axis=0, keepdims=True) * (1.0 / members)


def widen(block, width):
    return jnp.concatenate([block] * (width // block.shape[1]), axis=1)


def each_chunk(pixels, body, carry):
    def step(index, carry):
        return body(pl.ds(pl.multiple_of(index * CHUNK, CHUNK), CHUNK), carry)

    return lax.fori_loop(0, pixels // CHUNK, step, carry)


def norm_stats(read, pixels, channels):
    members = float(pixels * (channels // GROUPS))
    zeros = jnp.zeros((8, channels), jnp.float32)
    total = each_chunk(pixels, lambda rows, carry: carry + fold(read(rows)), zeros)
    mean = group_mean(total, members)

    def squares(rows, carry):
        centered = read(rows) - mean
        return carry + fold(centered * centered)

    spread = group_mean(each_chunk(pixels, squares, zeros), members)
    return mean, lax.rsqrt(spread + epsilon)


def put_taps(taps_ref, block, rows, cols):
    count, channels = block.shape
    place = lax.broadcasted_iota(jnp.int32, block.shape, 0) % cols
    left = jnp.where(place == 0, 0.0, pltpu.roll(block, 1, 0))
    right = jnp.where(place == cols - 1, 0.0, pltpu.roll(block, count - 1, 0))
    inner = pl.ds(pl.multiple_of(rows.start + cols, cols), count)
    taps_ref[inner, 0:channels] = left.astype(jnp.bfloat16)
    taps_ref[inner, channels : 2 * channels] = block.astype(jnp.bfloat16)
    taps_ref[inner, 2 * channels :] = right.astype(jnp.bfloat16)


def clear_edges(taps_ref, cols):
    edge = jnp.zeros((cols, taps_ref.shape[1]), taps_ref.dtype)
    taps_ref[0:cols, :] = edge
    taps_ref[taps_ref.shape[0] - cols :, :] = edge


def run_conv(taps_ref, product, mask_ref, total_ref, first, cols):
    pixels, channels = total_ref.shape
    block = min(CONV_ROWS, pixels)
    for row_tap in (1, 0, 2):

        def step(index, carry):
            start = pl.multiple_of(index * block, block)
            rows = pl.ds(start, block)
            shifted = pl.ds(pl.multiple_of(start + row_tap * cols, cols), block)
            part = product(taps_ref, shifted, row_tap)
            if row_tap == 1:
                total_ref[rows, :] = first(rows) + part
            else:
                total_ref[rows, :] += widen(mask_ref[row_tap // 2, rows, :], channels) * part
            return carry

        lax.fori_loop(0, pixels // block, step, 0)


def product_forward(weight_ref):
    channels = weight_ref.shape[-1]

    def product(taps_ref, shifted, row_tap):
        return jnp.dot(
            taps_ref[shifted, :],
            weight_ref[row_tap].reshape(3 * channels, channels),
            preferred_element_type=jnp.float32,
        )

    return product


def product_backward(weight_ref):
    channels = weight_ref.shape[-1]

    def product(taps_ref, shifted, row_tap):
        total = None
        for col_tap in range(3):
            part = lax.dot_general(
                taps_ref[shifted, col_tap * channels : (col_tap + 1) * channels],
                weight_ref[2 - row_tap, 2 - col_tap],
                (((1,), (1,)), ((), ())),
                preferred_element_type=jnp.float32,
            )
            total = part if total is None else total + part
        return total

    return product


def activate(read, which, stats, gains_ref, shifts_ref, act_ref, taps_ref, cols):
    mean, inverse = stats
    scale = inverse * gains_ref[which : which + 1, :]
    shift = shifts_ref[which : which + 1, :]

    def step(rows, carry):
        act = swish((read(rows) - mean) * scale + shift)
        act_ref[rows, :] = act.astype(jnp.bfloat16)
        put_taps(taps_ref, act, rows, cols)
        return carry

    each_chunk(act_ref.shape[0], step, 0)


def forward_kernel(
    features_ref,
    gains_ref,
    shifts_ref,
    biases_ref,
    mask_ref,
    weights_hbm,
    act_one_ref,
    middle_ref,
    act_two_ref,
    residual_ref,
    normed_ref,
    stats_ref,
    weights_ref,
    taps_ref,
    sems,
    *,
    cols,
):
    pixels, channels = features_ref.shape
    copies = [
        pltpu.make_async_copy(weights_hbm.at[which], weights_ref.at[which], sems.at[which])
        for which in range(2)
    ]
    for copy in copies:
        copy.start()
    clear_edges(taps_ref, cols)

    def read_input(rows):
        return features_ref[rows, :].astype(jnp.float32)

    def read_middle(rows):
        return middle_ref[rows, :]

    def read_residual(rows):
        return residual_ref[rows, :]

    stats = norm_stats(read_input, pixels, channels)
    stats_ref[0:1, :], stats_ref[1:2, :] = stats
    activate(read_input, 0, stats, gains_ref, shifts_ref, act_one_ref, taps_ref, cols)
    copies[0].wait()
    run_conv(
        taps_ref,
        product_forward(weights_ref.at[0]),
        mask_ref,
        middle_ref,
        lambda rows: biases_ref[0:1, :],
        cols,
    )
    stats = norm_stats(read_middle, pixels, channels)
    stats_ref[2:3, :], stats_ref[3:4, :] = stats
    activate(read_middle, 1, stats, gains_ref, shifts_ref, act_two_ref, taps_ref, cols)
    copies[1].wait()
    run_conv(
        taps_ref,
        product_forward(weights_ref.at[1]),
        mask_ref,
        residual_ref,
        lambda rows: read_input(rows) + biases_ref[1:2, :],
        cols,
    )
    mean, inverse = norm_stats(read_residual, pixels, channels)
    stats_ref[4:5, :], stats_ref[5:6, :] = mean, inverse
    scale = inverse * gains_ref[2:3, :]
    shift = shifts_ref[2:3, :]

    def finish(rows, carry):
        normed_ref[rows, :] = ((residual_ref[rows, :] - mean) * scale + shift).astype(jnp.bfloat16)
        return carry

    each_chunk(pixels, finish, 0)


def back_sums(read_pair, pixels, channels):
    zeros = jnp.zeros((8, channels), jnp.float32)

    def step(rows, carry):
        grad, normed = read_pair(rows)
        return carry[0] + fold(grad), carry[1] + fold(grad * normed)

    plain, cross = each_chunk(pixels, step, (zeros, zeros))
    return plain, cross


def back_means(sums, gain, pixels):
    channels = gain.shape[1]
    members = float(pixels * (channels // GROUPS))
    return group_mean(sums[0] * gain, members), group_mean(sums[1] * gain, members)


def column_total(partial):
    return jnp.sum(partial, axis=0, keepdims=True)


def attention_kernel(
    height_ref,
    normed_ref,
    residual_ref,
    grad_ref,
    qkv_ref,
    proj_ref,
    qv_bias_ref,
    proj_bias_ref,
    gains_ref,
    stats_ref,
    id_rows_ref,
    id_cols_ref,
    output_ref,
    mixed_ref,
    residual_grad_ref,
    grad_two_ref,
    sums_ref,
    query_ref,
    key_ref,
    value_ref,
    key_flip_ref,
    value_flip_ref,
    back_ref,
    out_flip_ref,
    packed_ref,
    key_sum_ref,
    value_sum_ref,
    flip_ref,
    *,
    score_scale,
):
    pixels, channels = normed_ref.shape
    own_pixels = output_ref.shape[0]
    share = mixed_ref.shape[0]
    height = height_ref[0]
    block = min(QUERY_ROWS, pixels)
    wide = jnp.float32

    def project(index, carry):
        rows = pl.ds(pl.multiple_of(index * block, block), block)
        normed = normed_ref[rows, :]
        query_ref[rows, :] = (
            jnp.dot(normed, qkv_ref[:, 0:channels], preferred_element_type=wide)
            + qv_bias_ref[0:1, :]
        ).astype(jnp.bfloat16)
        keys = jnp.dot(
            normed, qkv_ref[:, channels : 2 * channels], preferred_element_type=wide
        ).astype(jnp.bfloat16)
        values = (
            jnp.dot(normed, qkv_ref[:, 2 * channels :], preferred_element_type=wide)
            + qv_bias_ref[1:2, :]
        ).astype(jnp.bfloat16)
        key_ref[rows, :] = keys
        value_ref[rows, :] = values
        key_flip_ref[:, rows] = keys.T
        value_flip_ref[:, rows] = values.T
        back_ref[rows, :] = lax.dot_general(
            grad_ref[rows, :],
            proj_ref[...],
            (((1,), (1,)), ((), ())),
            preferred_element_type=wide,
        ).astype(jnp.bfloat16)
        return carry

    lax.fori_loop(0, pixels // block, project, 0)
    key_sum_ref[...] = jnp.zeros(key_sum_ref.shape, wide)
    value_sum_ref[...] = jnp.zeros(value_sum_ref.shape, wide)

    def attend(index, carry):
        rows = pl.ds(pl.multiple_of(index * block, block), block)
        queries = query_ref[rows, :]
        back = back_ref[rows, :]
        scores = lax.dot_general(
            key_ref[...], queries, (((1,), (1,)), ((), ())), preferred_element_type=wide
        )
        same = widen(id_rows_ref[...], block) == id_cols_ref[0:1, rows]
        scores = jnp.where(same, scores * score_scale, masked_score)
        scores = jnp.exp(scores - jnp.max(scores, axis=0, keepdims=True))
        weights = scores * (1.0 / jnp.sum(scores, axis=0, keepdims=True))
        rounded = weights.astype(jnp.bfloat16)
        out_flip_ref[:, rows] = jnp.dot(
            value_flip_ref[...], rounded, preferred_element_type=wide
        ).astype(jnp.bfloat16)
        value_sum_ref[...] += jnp.dot(rounded, back, preferred_element_type=wide)
        weight_grad = lax.dot_general(
            value_ref[...], back, (((1,), (1,)), ((), ())), preferred_element_type=wide
        )
        dots = jnp.sum(weights * weight_grad, axis=0, keepdims=True)
        score_grad = (weights * (weight_grad - dots)).astype(jnp.bfloat16)
        key_sum_ref[...] += jnp.dot(score_grad, queries, preferred_element_type=wide)
        query_grad = jnp.dot(key_flip_ref[...], score_grad, preferred_element_type=wide)
        packed_ref[rows, 0:channels] = (query_grad * score_scale).astype(jnp.bfloat16).T
        return carry

    lax.fori_loop(0, pixels // block, attend, 0)

    def pack(rows, carry):
        packed_ref[rows, channels : 2 * channels] = (key_sum_ref[rows, :] * score_scale).astype(
            jnp.bfloat16
        )
        packed_ref[rows, 2 * channels :] = value_sum_ref[rows, :].astype(jnp.bfloat16)
        return (
            carry[0] + fold(packed_ref[rows, 0:channels].astype(wide)),
            carry[1] + fold(packed_ref[rows, 2 * channels :].astype(wide)),
            carry[2] + fold(grad_ref[rows, :].astype(wide)),
        )

    zeros = jnp.zeros((8, channels), wide)
    query_total, value_total, grad_total = each_chunk(pixels, pack, (zeros, zeros, zeros))
    sums_ref[2:3, :] = column_total(query_total)
    sums_ref[3:4, :] = column_total(value_total)
    sums_ref[4:5, :] = column_total(grad_total)

    own = pl.ds(pl.multiple_of(height * own_pixels, own_pixels), own_pixels)
    output_ref[...] = (
        residual_ref[own, :]
        + lax.dot_general(
            out_flip_ref[:, own],
            proj_ref[...],
            (((0,), (0,)), ((), ())),
            preferred_element_type=wide,
        )
        + proj_bias_ref[...]
    ).astype(jnp.bfloat16)

    own_lanes = pl.ds(pl.multiple_of((height // 2) * (2 * share), 2 * share), 2 * share)
    flip_ref[...] = normed_ref[:, own_lanes].T
    own_share = pl.ds(pl.multiple_of((height % 2) * share, share), share)
    mixed_ref[:, 0 : 3 * channels] = jnp.dot(
        flip_ref[own_share, :], packed_ref[...], preferred_element_type=wide
    ).astype(jnp.bfloat16)
    own_out = pl.ds(pl.multiple_of(height * share, share), share)
    mixed_ref[:, 3 * channels :] = jnp.dot(
        out_flip_ref[own_out, :], grad_ref[...], preferred_element_type=wide
    ).astype(jnp.bfloat16)

    mean, inverse = stats_ref[4:5, :], stats_ref[5:6, :]
    gain = gains_ref[2:3, :]

    def input_grads(index, carry):
        rows = pl.ds(pl.multiple_of(index * block, block), block)
        normed_grad = lax.dot_general(
            packed_ref[rows, :],
            qkv_ref[...],
            (((1,), (1,)), ((), ())),
            preferred_element_type=wide,
        )
        key_sum_ref[rows, :] = normed_grad
        normed = (residual_ref[rows, :] - mean) * inverse
        return carry[0] + fold(normed_grad), carry[1] + fold(normed_grad * normed)

    sums = lax.fori_loop(0, pixels // block, input_grads, (zeros, zeros))
    sums_ref[0:1, :] = column_total(sums[1])
    sums_ref[1:2, :] = column_total(sums[0])
    mean_grad, mean_cross = back_means(sums, gain, pixels)

    def finish(rows, carry):
        normed = (residual_ref[rows, :] - mean) * inverse
        back = inverse * (key_sum_ref[rows, :] * gain - mean_grad - normed * mean_cross)
        total = grad_ref[rows, :].astype(wide) + back
        residual_grad_ref[rows, :] = total
        low = total.astype(jnp.bfloat16)
        grad_two_ref[rows, :] = low
        return carry + fold(low.astype(wide))

    sums_ref[5:6, :] = column_total(each_chunk(pixels, finish, zeros))


def weight_part(height, act_ref, grad_ref, mask_ref, narrow_ref, columns_ref, out_ref, cols):
    pixels, channels = act_ref.shape
    share = NARROW // 2
    block = pl.ds(pl.multiple_of((height // 2) * NARROW, NARROW), NARROW)
    parity = height % 2
    edge = jnp.zeros((cols, 3 * NARROW), jnp.float32)
    narrow_ref[0:cols, :] = edge
    narrow_ref[cols + pixels :, :] = edge

    def spread(rows, carry):
        own = grad_ref[rows, block].astype(jnp.float32)
        half = lax.broadcasted_iota(jnp.int32, own.shape, 1) // share
        turned = pltpu.roll(own, share, 1)
        both = jnp.where(half == parity, own, turned)
        place = lax.broadcasted_iota(jnp.int32, own.shape, 0) % cols
        left = jnp.where(place == 0, 0.0, pltpu.roll(both, 1, 0))
        right = jnp.where(place == cols - 1, 0.0, pltpu.roll(both, CHUNK - 1, 0))
        inner = pl.ds(pl.multiple_of(rows.start + cols, cols), CHUNK)
        narrow_ref[inner, 0:NARROW] = left
        narrow_ref[inner, NARROW : 2 * NARROW] = both
        narrow_ref[inner, 2 * NARROW :] = right
        return carry

    each_chunk(pixels, spread, 0)

    def gather(rows, carry):
        taps = []
        for row_tap in range(3):
            for col_tap in range(3):
                row_back, col_back = 2 - row_tap, 2 - col_tap
                shifted = pl.ds(pl.multiple_of(rows.start + row_back * cols, cols), CHUNK)
                block = narrow_ref[shifted, col_back * NARROW : (col_back + 1) * NARROW]
                if row_back != 1:
                    block = block * mask_ref[row_back // 2, rows, :]
                taps.append(block)
        lower = lax.broadcasted_iota(jnp.int32, taps[0].shape, 1) < share
        for pair in range(5):
            second = taps[min(2 * pair + 1, 8)]
            columns_ref[rows, pair * NARROW : (pair + 1) * NARROW] = jnp.where(
                lower, taps[2 * pair], second
            ).astype(jnp.bfloat16)
        return carry

    each_chunk(pixels, gather, 0)
    out_ref[...] = lax.dot_general(
        act_ref[...],
        columns_ref[...],
        (((0,), (0,)), ((), ())),
        preferred_element_type=jnp.float32,
    ).astype(jnp.bfloat16)


def conv_back(
    which, grad_ref, weights_ref, mask_ref, taps_ref, total_ref, read, stats, gains_ref, shifts_ref, cols
):
    pixels, channels = total_ref.shape
    wide = jnp.float32
    clear_edges(taps_ref, cols)

    def spread(rows, carry):
        put_taps(taps_ref, grad_ref[rows, :].astype(wide), rows, cols)
        return carry

    each_chunk(pixels, spread, 0)
    run_conv(
        taps_ref, product_backward(weights_ref), mask_ref, total_ref, lambda rows: 0.0, cols
    )
    mean, inverse = stats
    gain = gains_ref[which : which + 1, :]
    shift = shifts_ref[which : which + 1, :]

    def slope(rows):
        normed = (read(rows) - mean) * inverse
        grad = total_ref[rows, :] * swish_slope(normed * gain + shift)
        total_ref[rows, :] = grad
        return grad, normed

    sums = back_sums(slope, pixels, channels)
    mean_grad, mean_cross = back_means(sums, gain, pixels)

    def back(rows):
        normed = (read(rows) - mean) * inverse
        return inverse * (total_ref[rows, :] * gain - mean_grad - normed * mean_cross)

    return sums, back


def share_kernel(
    height_ref, act_ref, grad_ref, mask_ref, out_ref, narrow_ref, columns_ref, *, cols
):
    weight_part(
        height_ref[0], act_ref, grad_ref, mask_ref, narrow_ref, columns_ref, out_ref, cols
    )


def second_kernel(
    grad_two_ref,
    middle_ref,
    stats_ref,
    gains_ref,
    shifts_ref,
    mask_ref,
    weights_hbm,
    grad_one_ref,
    sums_ref,
    weights_ref,
    taps_ref,
    total_ref,
    sem,
    *,
    cols,
):
    pixels, channels = middle_ref.shape
    copy = pltpu.make_async_copy(weights_hbm.at[1], weights_ref, sem)
    copy.start()
    copy.wait()
    sums, back = conv_back(
        1,
        grad_two_ref,
        weights_ref,
        mask_ref,
        taps_ref,
        total_ref,
        lambda rows: middle_ref[rows, :],
        (stats_ref[2:3, :], stats_ref[3:4, :]),
        gains_ref,
        shifts_ref,
        cols,
    )
    sums_ref[0:1, :] = column_total(sums[1])
    sums_ref[1:2, :] = column_total(sums[0])

    def finish(rows, carry):
        low = back(rows).astype(jnp.bfloat16)
        grad_one_ref[rows, :] = low
        return carry + fold(low.astype(jnp.float32))

    zeros = jnp.zeros((8, channels), jnp.float32)
    sums_ref[2:3, :] = column_total(each_chunk(pixels, finish, zeros))


def first_kernel(
    height_ref,
    grad_one_ref,
    features_ref,
    residual_grad_ref,
    stats_ref,
    gains_ref,
    shifts_ref,
    mask_ref,
    weights_hbm,
    input_grad_ref,
    sums_ref,
    weights_ref,
    taps_ref,
    total_ref,
    sem,
    *,
    cols,
):
    copy = pltpu.make_async_copy(weights_hbm.at[0], weights_ref, sem)
    copy.start()
    copy.wait()
    sums, back = conv_back(
        0,
        grad_one_ref,
        weights_ref,
        mask_ref,
        taps_ref,
        total_ref,
        lambda rows: features_ref[rows, :].astype(jnp.float32),
        (stats_ref[0:1, :], stats_ref[1:2, :]),
        gains_ref,
        shifts_ref,
        cols,
    )
    sums_ref[0:1, :] = column_total(sums[1])
    sums_ref[1:2, :] = column_total(sums[0])
    count = input_grad_ref.shape[0]
    own = pl.ds(pl.multiple_of(height_ref[0] * count, count), count)
    input_grad_ref[...] = (residual_grad_ref[own, :] + back(own)).astype(jnp.bfloat16)


def join_kernel(*refs):
    out_ref = refs[-1]
    share = out_ref.shape[-1]
    for which in range(2):
        parts = refs[which * (len(refs) - 1) // 2 : (which + 1) * (len(refs) - 1) // 2]
        total = parts[0][...].astype(jnp.float32)
        for part in parts[1:]:
            total = total + part[...].astype(jnp.float32)
        for tap in range(9):
            out_ref[which, tap // 3, tap % 3] = total[:, tap * share : (tap + 1) * share]


def call_kernel(kernel, outputs, scratch, operands, places, flops):
    spaces = {
        "v": pl.BlockSpec(memory_space=pltpu.VMEM),
        "s": pl.BlockSpec(memory_space=pltpu.SMEM),
        "h": pl.BlockSpec(memory_space=pl.ANY),
    }
    moved = sum(array.size * array.dtype.itemsize for array in operands)
    return pl.pallas_call(
        kernel,
        out_shape=[jax.ShapeDtypeStruct(shape, dtype) for shape, dtype in outputs],
        in_specs=[spaces[place] for place in places],
        out_specs=[spaces["v"]] * len(outputs),
        scratch_shapes=scratch,
        compiler_params=pltpu.CompilerParams(vmem_limit_bytes=VMEM_BYTES),
        cost_estimate=pl.CostEstimate(flops=flops, bytes_accessed=moved, transcendentals=0),
    )(*operands)


def exchange(part, share):
    size = lax.axis_size("canvas")
    me = lax.axis_index("canvas")
    pieces = [lax.dynamic_slice_in_dim(part, me * share, share)]
    for step in range(1, size):
        if size & (size - 1) == 0:
            pairs = [(i, i ^ step) for i in range(size)]
            target = me ^ step
        else:
            pairs = [(i, (i + step) % size) for i in range(size)]
            target = (me + step) % size
        sent = lax.dynamic_slice_in_dim(part, target * share, share)
        pieces.append(lax.ppermute(sent, "canvas", pairs))
    return pieces


def add_pieces(pieces):
    total = pieces[0].astype(jnp.float32)
    for piece in pieces[1:]:
        total = total + piece.astype(jnp.float32)
    return total


def whole_canvas(
    features,
    tile_ids,
    norm_gains,
    norm_shifts,
    conv_weights,
    conv_biases,
    qkv_weight,
    qv_bias,
    proj_weight,
    proj_bias,
    cotangent,
):
    height_size = lax.axis_size("height")
    canvas_size = lax.axis_size("canvas")
    local_rows, cols, channels = features.shape[1:]
    row_ids = tile_ids[0]
    all_rows = row_ids.shape[0]
    pixels = all_rows * cols
    own_pixels = local_rows * cols
    out_share = channels // height_size
    low, wide = jnp.bfloat16, jnp.float32
    height = lax.axis_index("height").reshape(1)

    all_features = lax.all_gather(features[0], "height", axis=0, tiled=True)
    late_cotangent, all_features = lax.optimization_barrier((cotangent[0], all_features))
    out_grad = lax.all_gather(late_cotangent, "height", axis=0, tiled=True)
    out_grad = out_grad.reshape(pixels, channels)
    all_features = all_features.reshape(pixels, channels)

    edge_ids = jnp.full((1,), -1, jnp.int32)
    padded_ids = jnp.concatenate([edge_ids, row_ids, edge_ids])
    row_mask = jnp.stack(
        [padded_ids[:all_rows] == row_ids, padded_ids[2:] == row_ids], axis=0
    ).astype(wide)
    mask = jnp.broadcast_to(jnp.repeat(row_mask, cols, axis=1)[:, :, None], (2, pixels, LANES))
    pixel_ids = jnp.repeat(row_ids, cols)
    id_rows = jnp.broadcast_to(pixel_ids[:, None], (pixels, LANES))
    id_cols = jnp.broadcast_to(pixel_ids[None, :], (8, pixels))

    plane = ((pixels, channels), low)
    plane_wide = ((pixels, channels), wide)
    rows_wide = ((8, channels), wide)
    taps = pltpu.VMEM((pixels + 2 * cols, 3 * channels), low)
    one_sem = pltpu.SemaphoreType.DMA
    conv_flops = 2 * 9 * pixels * channels * channels

    act_one, middle, act_two, residual, normed, stats = call_kernel(
        functools.partial(forward_kernel, cols=cols),
        [plane, plane_wide, plane, plane_wide, plane, rows_wide],
        [pltpu.VMEM(conv_weights.shape, low), taps, pltpu.SemaphoreType.DMA((2,))],
        [all_features, norm_gains, norm_shifts, conv_biases, mask, conv_weights],
        "vvvvvh",
        2 * conv_flops,
    )
    output, mixed, residual_grad, grad_two, sums_three = call_kernel(
        functools.partial(attention_kernel, score_scale=channels ** (-0.5)),
        [
            ((own_pixels, channels), low),
            ((out_share, 4 * channels), low),
            plane_wide,
            plane,
            rows_wide,
        ],
        [
            pltpu.VMEM((pixels, channels), low),
            pltpu.VMEM((pixels, channels), low),
            pltpu.VMEM((pixels, channels), low),
            pltpu.VMEM((channels, pixels), low),
            pltpu.VMEM((channels, pixels), low),
            pltpu.VMEM((pixels, channels), low),
            pltpu.VMEM((channels, pixels), low),
            pltpu.VMEM((pixels, 3 * channels), low),
            pltpu.VMEM((pixels, channels), wide),
            pltpu.VMEM((pixels, channels), wide),
            pltpu.VMEM((2 * out_share, pixels), low),
        ],
        [
            height,
            normed,
            residual,
            out_grad,
            qkv_weight,
            proj_weight,
            qv_bias,
            proj_bias.reshape(1, channels),
            norm_gains,
            stats,
            id_rows,
            id_cols,
        ],
        "svvvvvvvvvvv",
        10 * pixels * channels * channels + 12 * pixels * pixels * channels,
    )
    mixed_sum = add_pieces(exchange(mixed, out_share // canvas_size))
    mixed_grad = lax.all_gather(mixed_sum.astype(low), ("height", "canvas"), axis=0, tiled=True)
    qkv_grad = mixed_grad[:, : 3 * channels].astype(wide)
    proj_grad = mixed_grad[:, 3 * channels :].astype(wide)

    def weight_share(act, grad):
        (part,) = call_kernel(
            functools.partial(share_kernel, cols=cols),
            [((channels, 5 * LANES), low)],
            [
                pltpu.VMEM((pixels + 2 * cols, 3 * LANES), wide),
                pltpu.VMEM((pixels, 5 * LANES), low),
            ],
            [height, act, grad, mask],
            "svvv",
            conv_flops // height_size,
        )
        return exchange(part, channels // canvas_size)

    parts_two = weight_share(act_two, grad_two)
    back_scratch = [
        pltpu.VMEM(conv_weights.shape[1:], low),
        taps,
        pltpu.VMEM((pixels, channels), wide),
        one_sem,
    ]
    grad_one, sums_two = call_kernel(
        functools.partial(second_kernel, cols=cols),
        [plane, rows_wide],
        back_scratch,
        [grad_two, middle, stats, norm_gains, norm_shifts, mask, conv_weights],
        "vvvvvvh",
        conv_flops,
    )
    parts_one = weight_share(act_one, grad_one)
    input_grad, sums_one = call_kernel(
        functools.partial(first_kernel, cols=cols),
        [((own_pixels, channels), low), rows_wide],
        back_scratch,
        [
            height,
            grad_one,
            all_features,
            residual_grad,
            stats,
            norm_gains,
            norm_shifts,
            mask,
            conv_weights,
        ],
        "svvvvvvvh",
        conv_flops,
    )
    (conv_grad,) = call_kernel(
        join_kernel,
        [((2, 3, 3, channels // canvas_size, out_share), wide)],
        [],
        parts_one + parts_two,
        "v" * (len(parts_one) + len(parts_two)),
        0,
    )
    sums = jnp.concatenate([sums_one, sums_two, sums_three], axis=0)
    total = sums
    for step in range(1, canvas_size):
        pairs = [(i, (i + step) % canvas_size) for i in range(canvas_size)]
        total = total + lax.ppermute(sums, "canvas", pairs)
    one, two, three = 0, 8, 16
    own_shape = (1, local_rows, cols, channels)
    return (
        output.reshape(own_shape),
        input_grad.reshape(own_shape),
        jnp.stack([total[one], total[two], total[three]]),
        jnp.stack([total[one + 1], total[two + 1], total[three + 1]]),
        conv_grad,
        jnp.stack([total[two + 2], total[three + 5]]),
        qkv_grad,
        jnp.stack([total[three + 2], total[three + 3]]),
        proj_grad,
        total[three + 4],
    )


def on_device(*arrays):
    features, tile_ids = arrays[0], arrays[1]
    local_rows, cols, channels = features.shape[1:]
    height_size, canvas_size = lax.axis_size("height"), lax.axis_size("canvas")
    fits = (
        tile_ids.shape[1] * cols <= MOST_PIXELS
        and (tile_ids.shape[1] * cols) % (2 * CHUNK) == 0
        and (local_rows * cols) % LANES == 0
        and CHUNK % cols == 0
        and cols % 16 == 0
        and channels % (2 * LANES) == 0
        and 2 * channels == LANES * height_size
        and channels % (16 * canvas_size) == 0
    )
    return whole_canvas(*arrays) if fits else split_canvas(*arrays)


def solution(mesh):
    in_specs = (
        P("canvas", "height", None, None),
        P("canvas", None),
        P(),
        P(),
        P(),
        P(),
        P(),
        P(),
        P(),
        P(),
        P("canvas", "height", None, None),
    )
    out_specs = (
        P("canvas", "height", None, None),
        P("canvas", "height", None, None),
        P(),
        P(),
        P(None, None, None, "canvas", "height"),
        P(),
        P(),
        P(),
        P(),
        P(),
    )
    return jax.shard_map(
        on_device, mesh=mesh, in_specs=in_specs, out_specs=out_specs, check_vma=False
    )
```

```python
import functools

import jax
import jax.numpy as jnp
from jax import lax
from jax.experimental import pallas as pl
from jax.experimental.pallas import tpu as pltpu
from jax.sharding import PartitionSpec as P

GROUPS = 32


epsilon = 1e-06
masked_score = -1e30
MOST_PIXELS = 1024
LANES = 128
NARROW = 128
CHUNK = 128
CONV_ROWS = 512
QUERY_ROWS = 256


def extended(block, sides, width):
    for axis, dim in sides:
        count = lax.axis_size(axis)
        forward = [(i, i + 1) for i in range(count - 1)]
        backward = [(target, source) for source, target in forward]
        low = lax.ppermute(
            lax.slice_in_dim(block, block.shape[dim] - width, None, axis=dim), axis, forward
        )
        high = lax.ppermute(lax.slice_in_dim(block, 0, width, axis=dim), axis, backward)
        block = jnp.concatenate([low, block, high], axis=dim)
    return block


def group_total(vector):
    return vector.reshape(GROUPS, -1).sum(axis=1)


def spread_groups(vector, channels):
    return jnp.repeat(vector, channels // GROUPS)


def norm_forward(values, gain, shift, members):
    channels = values.shape[1]
    totals = lax.psum(group_total(jnp.sum(values, axis=0)), "height")
    centered = values - spread_groups(totals / members, channels)
    squares = lax.psum(group_total(jnp.sum(centered * centered, axis=0)), "height")
    inverse = spread_groups(lax.rsqrt(squares / members + epsilon), channels)
    normed = centered * inverse
    return (normed, inverse, normed * gain + shift)


def norm_backward(grad_in, normed, inverse, gain, members):
    channels = grad_in.shape[1]
    scaled = grad_in * gain
    both_sums = lax.psum(
        (group_total(jnp.sum(scaled, axis=0)), group_total(jnp.sum(scaled * normed, axis=0))),
        "height",
    )
    mean_grad = spread_groups(both_sums[0] / members, channels)
    mean_cross = spread_groups(both_sums[1] / members, channels)
    result = inverse * (scaled - mean_grad - normed * mean_cross)
    return (result, jnp.sum(grad_in * normed, axis=0), jnp.sum(grad_in, axis=0))


def swish(values):
    return values * jax.nn.sigmoid(values)


def swish_slope(values):
    sigmoid_part = jax.nn.sigmoid(values)
    return sigmoid_part * (1.0 + values * (1.0 - sigmoid_part))


def tap_columns(padded, row_mask, local_rows, canvas_cols):
    pieces = []
    for row_tap in range(3):
        rows_taken = padded[row_tap : row_tap + local_rows] * row_mask[:, row_tap, None, None]
        for col_tap in range(3):
            pieces.append(rows_taken[:, col_tap : col_tap + canvas_cols])
    stacked = jnp.concatenate(pieces, axis=2)
    return stacked.reshape(local_rows * canvas_cols, stacked.shape[2])


def conv_forward(acts, row_mask, weight, bias):
    local_rows, canvas_cols, channels = acts.shape
    rimmed = extended(acts, (("height", 0),), 1)
    padded = jnp.pad(rimmed, ((0, 0), (1, 1), (0, 0)))
    gathered = tap_columns(padded, row_mask, local_rows, canvas_cols)
    result = (
        jnp.dot(
            gathered, weight.reshape(9 * channels, channels), preferred_element_type=jnp.float32
        )
        + bias
    )
    return (result, gathered)


def conv_backward(grad_low, row_mask, weight, gathered):
    local_rows, canvas_cols, channels = grad_low.shape
    flat_grad = grad_low.reshape(local_rows * canvas_cols, channels)
    weight_grad = lax.dot_general(
        gathered, flat_grad, (((0,), (0,)), ((), ())), preferred_element_type=jnp.float32
    )
    rimmed = extended(grad_low, (("height", 0),), 1)
    padded = jnp.pad(rimmed, ((0, 0), (1, 1), (0, 0)))
    grad_taps = tap_columns(padded, row_mask, local_rows, canvas_cols)
    flipped = jnp.transpose(weight[::-1, ::-1], (0, 1, 3, 2)).reshape(9 * channels, channels)
    input_part = jnp.dot(grad_taps, flipped, preferred_element_type=jnp.float32)
    return (
        input_part,
        weight_grad.reshape(3, 3, channels, channels),
        jnp.sum(flat_grad.astype(jnp.float32), axis=0),
    )


def take_rows(array, offset, count):
    return lax.dynamic_slice_in_dim(array, offset, count)


def score_grads(
    queries, out_grad, log_total, row_dots, query_ids, key_rows, value_rows, key_ids, score_scale
):
    scores = (
        lax.dot_general(
            queries, key_rows, (((1,), (1,)), ((), ())), preferred_element_type=jnp.float32
        )
        * score_scale
    )
    same_tile = query_ids[:, None] == key_ids[None, :]
    softmax_block = jnp.exp(jnp.where(same_tile, scores - log_total[:, None], masked_score))
    weight_grad = lax.dot_general(
        out_grad, value_rows, (((1,), (1,)), ((), ())), preferred_element_type=jnp.float32
    )
    score_grad = (softmax_block * (weight_grad - row_dots[:, None])).astype(jnp.bfloat16)
    return (softmax_block.astype(jnp.bfloat16), score_grad)


def split_canvas(
    features,
    tile_ids,
    norm_gains,
    norm_shifts,
    conv_weights,
    conv_biases,
    qkv_weight,
    qv_bias,
    proj_weight,
    proj_bias,
    cotangent,
):
    height_size = lax.axis_size("height")
    local_rows = features.shape[1]
    canvas_cols = features.shape[2]
    channels = features.shape[3]
    pixels = local_rows * canvas_cols
    row_ids = tile_ids[0]
    all_rows = row_ids.shape[0]
    members = float(all_rows * canvas_cols * (channels // GROUPS))
    score_scale = channels ** (-0.5)
    first_row = lax.axis_index("height") * local_rows
    edge_ids = jnp.full((1,), -1, jnp.int32)
    padded_ids = jnp.concatenate([edge_ids, row_ids, edge_ids])
    near_ids = lax.dynamic_slice_in_dim(padded_ids, first_row, local_rows + 2)
    own_rows = near_ids[1 : local_rows + 1]
    row_mask = jnp.stack(
        [near_ids[row_tap : row_tap + local_rows] == own_rows for row_tap in range(3)], axis=1
    ).astype(jnp.bfloat16)
    key_ids = jnp.repeat(row_ids, canvas_cols)
    query_ids = jnp.repeat(own_rows, canvas_cols)
    grid_shape = (local_rows, canvas_cols, channels)
    inputs = features[0].reshape(pixels, channels).astype(jnp.float32)
    normed_one, inverse_one, pre_one = norm_forward(inputs, norm_gains[0], norm_shifts[0], members)
    act_one = swish(pre_one).astype(jnp.bfloat16).reshape(grid_shape)
    middle, taps_one = conv_forward(act_one, row_mask, conv_weights[0], conv_biases[0])
    normed_two, inverse_two, pre_two = norm_forward(middle, norm_gains[1], norm_shifts[1], members)
    act_two = swish(pre_two).astype(jnp.bfloat16).reshape(grid_shape)
    branch, taps_two = conv_forward(act_two, row_mask, conv_weights[1], conv_biases[1])
    residual = inputs + branch
    normed_three, inverse_three, pre_three = norm_forward(
        residual, norm_gains[2], norm_shifts[2], members
    )
    attn_input = pre_three.astype(jnp.bfloat16)
    mixed = jnp.dot(attn_input, qkv_weight, preferred_element_type=jnp.float32)
    queries = (mixed[:, :channels] + qv_bias[0]).astype(jnp.bfloat16)
    key_rows = mixed[:, channels : 2 * channels].astype(jnp.bfloat16)
    value_rows = (mixed[:, 2 * channels :] + qv_bias[1]).astype(jnp.bfloat16)
    running_max = jnp.full((pixels,), masked_score, jnp.float32)
    key_piece = lax.all_gather(key_rows, "height", axis=0, tiled=True)
    value_piece = lax.all_gather(value_rows, "height", axis=0, tiled=True)
    scores = (
        lax.dot_general(
            queries, key_piece, (((1,), (1,)), ((), ())), preferred_element_type=jnp.float32
        )
        * score_scale
    )
    same_tile = query_ids[:, None] == key_ids[None, :]
    scores = jnp.where(same_tile, scores, masked_score)
    new_max = jnp.maximum(running_max, jnp.max(scores, axis=1))
    weights = jnp.where(same_tile, jnp.exp(scores - new_max[:, None]), 0.0)
    summed_out = jnp.dot(
        weights.astype(jnp.bfloat16), value_piece, preferred_element_type=jnp.float32
    )
    total_weight = jnp.sum(weights, axis=1)
    log_total = new_max + jnp.log(total_weight)
    attended = summed_out / total_weight[:, None]
    attended_low = attended.astype(jnp.bfloat16)
    output = (
        residual
        + jnp.dot(attended_low, proj_weight, preferred_element_type=jnp.float32)
        + proj_bias
    )
    out_grad = cotangent[0].reshape(pixels, channels)
    out_grad_full = out_grad.astype(jnp.float32)
    proj_grad = lax.dot_general(
        attended_low, out_grad, (((0,), (0,)), ((), ())), preferred_element_type=jnp.float32
    )
    proj_bias_grad = jnp.sum(out_grad_full, axis=0)
    attended_grad = lax.dot_general(
        out_grad, proj_weight, (((1,), (1,)), ((), ())), preferred_element_type=jnp.float32
    ).astype(jnp.bfloat16)
    row_dots = jnp.sum(attended_grad.astype(jnp.float32) * attended, axis=1)
    block_rows = pixels * min(height_size, 8)
    zero_block = jnp.zeros((pixels, channels), jnp.float32)
    key_all, value_all = (
        lax.all_gather(key_rows, "height", axis=0, tiled=True),
        lax.all_gather(value_rows, "height", axis=0, tiled=True),
    )
    query_all, grad_all = (
        lax.all_gather(queries, "height", axis=0, tiled=True),
        lax.all_gather(attended_grad, "height", axis=0, tiled=True),
    )
    total_all, dots_all = (
        lax.all_gather(log_total, "height", axis=0, tiled=True),
        lax.all_gather(row_dots, "height", axis=0, tiled=True),
    )

    def own_query_step(running, block_index):
        offset = block_index * block_rows
        key_part = take_rows(key_all, offset, block_rows)
        rounded, score_grad = score_grads(
            queries,
            attended_grad,
            log_total,
            row_dots,
            query_ids,
            key_part,
            take_rows(value_all, offset, block_rows),
            take_rows(key_ids, offset, block_rows),
            score_scale,
        )
        return (
            running
            + jnp.dot(score_grad, key_part, preferred_element_type=jnp.float32) * score_scale,
            None,
        )

    def own_key_step(running, block_index):
        offset = block_index * block_rows
        query_part = take_rows(query_all, offset, block_rows)
        grad_part = take_rows(grad_all, offset, block_rows)
        rounded, score_grad = score_grads(
            query_part,
            grad_part,
            take_rows(total_all, offset, block_rows),
            take_rows(dots_all, offset, block_rows),
            take_rows(key_ids, offset, block_rows),
            key_rows,
            value_rows,
            query_ids,
            score_scale,
        )
        key_part = (
            lax.dot_general(
                score_grad, query_part, (((0,), (0,)), ((), ())), preferred_element_type=jnp.float32
            )
            * score_scale
        )
        value_part = lax.dot_general(
            rounded, grad_part, (((0,), (0,)), ((), ())), preferred_element_type=jnp.float32
        )
        return ((running[0] + key_part, running[1] + value_part), None)

    block_count = key_all.shape[0] // block_rows
    query_grad, unused_one = lax.scan(own_query_step, zero_block, jnp.arange(block_count))
    (key_grad, value_grad), unused_two = lax.scan(
        own_key_step, (zero_block, zero_block), jnp.arange(block_count)
    )
    query_low = query_grad.astype(jnp.bfloat16)
    key_low = key_grad.astype(jnp.bfloat16)
    value_low = value_grad.astype(jnp.bfloat16)
    stacked_grad = jnp.concatenate([query_low, key_low, value_low], axis=1)
    qkv_grad = lax.dot_general(
        attn_input, stacked_grad, (((0,), (0,)), ((), ())), preferred_element_type=jnp.float32
    )
    qv_grad = jnp.stack(
        [
            jnp.sum(query_low.astype(jnp.float32), axis=0),
            jnp.sum(value_low.astype(jnp.float32), axis=0),
        ]
    )
    normed_grad = lax.dot_general(
        stacked_grad, qkv_weight, (((1,), (1,)), ((), ())), preferred_element_type=jnp.float32
    )
    back_three, gain_three, shift_three = norm_backward(
        normed_grad, normed_three, inverse_three, norm_gains[2], members
    )
    residual_grad = out_grad_full + back_three
    grad_two = residual_grad.astype(jnp.bfloat16).reshape(grid_shape)
    act_two_grad, weight_two_grad, bias_two_grad = conv_backward(
        grad_two, row_mask, conv_weights[1], taps_two
    )
    middle_grad, gain_two, shift_two = norm_backward(
        act_two_grad * swish_slope(pre_two), normed_two, inverse_two, norm_gains[1], members
    )
    grad_one = middle_grad.astype(jnp.bfloat16).reshape(grid_shape)
    act_one_grad, weight_one_grad, bias_one_grad = conv_backward(
        grad_one, row_mask, conv_weights[0], taps_one
    )
    input_back, gain_one, shift_one = norm_backward(
        act_one_grad * swish_slope(pre_one), normed_one, inverse_one, norm_gains[0], members
    )
    input_grad = residual_grad + input_back
    conv_grad = jnp.stack([weight_one_grad, weight_two_grad])
    conv_part = lax.psum_scatter(conv_grad, "height", scatter_dimension=4, tiled=True)
    conv_part = lax.psum_scatter(
        conv_part.astype(jnp.bfloat16), "canvas", scatter_dimension=3, tiled=True
    ).astype(jnp.float32)
    summed = lax.psum(
        (
            jnp.stack([gain_one, gain_two, gain_three]),
            jnp.stack([shift_one, shift_two, shift_three]),
            jnp.stack([bias_one_grad, bias_two_grad]),
            qkv_grad,
            qv_grad,
            proj_grad,
            proj_bias_grad,
        ),
        ("canvas", "height"),
    )
    return (
        output.astype(jnp.bfloat16).reshape((1,) + grid_shape),
        input_grad.astype(jnp.bfloat16).reshape((1,) + grid_shape),
        summed[0],
        summed[1],
        conv_part,
        summed[2],
        summed[3],
        summed[4],
        summed[5],
        summed[6],
    )


def fold(block):
    rows, width = block.shape
    return jnp.sum(block.reshape(rows // 8, 8, width), axis=0)


def group_lanes(block, group):
    lane = lax.broadcasted_iota(jnp.int32, block.shape, 1)
    width = block.shape[1]
    step = 1
    while step < group:
        above = pltpu.roll(block, step, 1)
        below = pltpu.roll(block, width - step, 1)
        block = block + jnp.where((lane & step) != 0, above, below)
        step *= 2
    return block


def group_mean(partial, members):
    spread = group_lanes(partial, partial.shape[1] // GROUPS)
    return jnp.sum(spread, axis=0, keepdims=True) * (1.0 / members)


def widen(block, width):
    return jnp.concatenate([block] * (width // block.shape[1]), axis=1)


def each_chunk(pixels, body, carry):
    def step(index, carry):
        return body(pl.ds(pl.multiple_of(index * CHUNK, CHUNK), CHUNK), carry)

    return lax.fori_loop(0, pixels // CHUNK, step, carry)


def norm_stats(read, pixels, channels):
    members = float(pixels * (channels // GROUPS))
    zeros = jnp.zeros((8, channels), jnp.float32)
    total = each_chunk(pixels, lambda rows, carry: carry + fold(read(rows)), zeros)
    mean = group_mean(total, members)

    def squares(rows, carry):
        centered = read(rows) - mean
        return carry + fold(centered * centered)

    spread = group_mean(each_chunk(pixels, squares, zeros), members)
    return mean, lax.rsqrt(spread + epsilon)


def put_taps(taps_ref, block, rows, cols):
    count, channels = block.shape
    place = lax.broadcasted_iota(jnp.int32, block.shape, 0) & (cols - 1)
    left = jnp.where(place == 0, 0.0, pltpu.roll(block, 1, 0))
    right = jnp.where(place == cols - 1, 0.0, pltpu.roll(block, count - 1, 0))
    inner = pl.ds(pl.multiple_of(rows.start + cols, cols), count)
    taps_ref[inner, 0:channels] = left.astype(jnp.bfloat16)
    taps_ref[inner, channels : 2 * channels] = block.astype(jnp.bfloat16)
    taps_ref[inner, 2 * channels :] = right.astype(jnp.bfloat16)


def clear_edges(taps_ref, cols):
    edge = jnp.zeros((cols, taps_ref.shape[1]), taps_ref.dtype)
    taps_ref[0:cols, :] = edge
    taps_ref[taps_ref.shape[0] - cols :, :] = edge


def run_conv(taps_ref, product, mask_ref, total_ref, first, cols):
    pixels, channels = total_ref.shape
    block = min(CONV_ROWS, pixels)
    for row_tap in (1, 0, 2):

        def step(index, carry):
            start = pl.multiple_of(index * block, block)
            rows = pl.ds(start, block)
            shifted = pl.ds(pl.multiple_of(start + row_tap * cols, cols), block)
            part = product(taps_ref, shifted, row_tap)
            if row_tap == 1:
                total_ref[rows, :] = first(rows) + part
            else:
                total_ref[rows, :] += widen(mask_ref[row_tap // 2, rows, :], channels) * part
            return carry

        lax.fori_loop(0, pixels // block, step, 0)


def product_forward(weight_ref):
    channels = weight_ref.shape[-1]

    def product(taps_ref, shifted, row_tap):
        return jnp.dot(
            taps_ref[shifted, :],
            weight_ref[row_tap].reshape(3 * channels, channels),
            preferred_element_type=jnp.float32,
        )

    return product


def product_backward(weight_ref):
    channels = weight_ref.shape[-1]

    def product(taps_ref, shifted, row_tap):
        total = None
        for col_tap in range(3):
            part = lax.dot_general(
                taps_ref[shifted, col_tap * channels : (col_tap + 1) * channels],
                weight_ref[2 - row_tap, 2 - col_tap],
                (((1,), (1,)), ((), ())),
                preferred_element_type=jnp.float32,
            )
            total = part if total is None else total + part
        return total

    return product


def smooth(values):
    part = 0.5 * jnp.tanh(0.5 * values) + 0.5
    return values * part, part


def activate(read, mean, inverse, gain, shift, act_ref, taps_ref, cols):
    scale = inverse * gain

    def step(rows, carry):
        act = smooth((read(rows) - mean) * scale + shift)[0]
        act_ref[rows, :] = act.astype(jnp.bfloat16)
        put_taps(taps_ref, act, rows, cols)
        return carry

    each_chunk(act_ref.shape[0], step, 0)


def back_sums(read_pair, pixels, channels):
    zeros = jnp.zeros((8, channels), jnp.float32)

    def step(rows, carry):
        grad, normed = read_pair(rows)
        return carry[0] + fold(grad), carry[1] + fold(grad * normed)

    plain, cross = each_chunk(pixels, step, (zeros, zeros))
    return plain, cross


def back_means(sums, gain, pixels):
    channels = gain.shape[1]
    members = float(pixels * (channels // GROUPS))
    return group_mean(sums[0] * gain, members), group_mean(sums[1] * gain, members)


def column_total(partial):
    return jnp.sum(partial, axis=0, keepdims=True)


def weight_part(height, act_ref, grad_ref, mask_ref, narrow_ref, columns_ref, out_ref, cols):
    pixels, channels = act_ref.shape
    share = NARROW // 2
    block = pl.ds(pl.multiple_of((height // 2) * NARROW, NARROW), NARROW)
    parity = height % 2
    edge = jnp.zeros((cols, 3 * NARROW), jnp.float32)
    narrow_ref[0:cols, :] = edge
    narrow_ref[cols + pixels :, :] = edge

    def spread(rows, carry):
        own = grad_ref[rows, block].astype(jnp.float32)
        half = lax.broadcasted_iota(jnp.int32, own.shape, 1) // share
        turned = pltpu.roll(own, share, 1)
        both = jnp.where(half == parity, own, turned)
        place = lax.broadcasted_iota(jnp.int32, own.shape, 0) & (cols - 1)
        left = jnp.where(place == 0, 0.0, pltpu.roll(both, 1, 0))
        right = jnp.where(place == cols - 1, 0.0, pltpu.roll(both, CHUNK - 1, 0))
        inner = pl.ds(pl.multiple_of(rows.start + cols, cols), CHUNK)
        narrow_ref[inner, 0:NARROW] = left
        narrow_ref[inner, NARROW : 2 * NARROW] = both
        narrow_ref[inner, 2 * NARROW :] = right
        return carry

    each_chunk(pixels, spread, 0)

    def gather(rows, carry):
        taps = []
        for row_tap in range(3):
            for col_tap in range(3):
                row_back, col_back = 2 - row_tap, 2 - col_tap
                shifted = pl.ds(pl.multiple_of(rows.start + row_back * cols, cols), CHUNK)
                block = narrow_ref[shifted, col_back * NARROW : (col_back + 1) * NARROW]
                if row_back != 1:
                    block = block * mask_ref[row_back // 2, rows, :]
                taps.append(block)
        lower = lax.broadcasted_iota(jnp.int32, taps[0].shape, 1) < share
        for pair in range(5):
            second = taps[min(2 * pair + 1, 8)]
            columns_ref[rows, pair * NARROW : (pair + 1) * NARROW] = jnp.where(
                lower, taps[2 * pair], second
            ).astype(jnp.bfloat16)
        return carry

    each_chunk(pixels, gather, 0)
    part = lax.dot_general(
        columns_ref[...],
        act_ref[...],
        (((0,), (0,)), ((), ())),
        preferred_element_type=jnp.float32,
    ).astype(jnp.bfloat16)
    pieces, rows, width = out_ref.shape
    for piece in range(pieces):
        out_ref[piece] = part[0:rows, piece * width : (piece + 1) * width]


def conv_back(grad_ref, copy, weights_ref, mask_ref, taps_ref, total_ref, read, table_ref, which, cols):
    pixels, channels = total_ref.shape
    wide = jnp.float32
    clear_edges(taps_ref, cols)

    def spread(rows, carry):
        put_taps(taps_ref, grad_ref[rows, :].astype(wide), rows, cols)
        return carry

    each_chunk(pixels, spread, 0)
    copy.wait()
    run_conv(
        taps_ref, product_backward(weights_ref), mask_ref, total_ref, lambda rows: 0.0, cols
    )
    mean, inverse, gain, shift = norm_rows(table_ref, which)

    def slope(rows):
        normed = (read(rows) - mean) * inverse
        pre = normed * gain + shift
        part = smooth(pre)[1]
        grad = total_ref[rows, :] * (part * (1.0 + pre * (1.0 - part)))
        total_ref[rows, :] = grad
        return grad, normed

    sums = back_sums(slope, pixels, channels)
    mean_grad, mean_cross = back_means(sums, gain, pixels)

    def back(rows):
        normed = (read(rows) - mean) * inverse
        return inverse * (total_ref[rows, :] * gain - mean_grad - normed * mean_cross)

    return sums, back


def norm_rows(table_ref, which):
    picks = (2 * which, 2 * which + 1, 6 + which, 9 + which)
    return tuple(table_ref[pick : pick + 1, :] for pick in picks)


def build_masks(ids_ref, mask_ref, id_rows_ref, id_cols_ref, cols):
    rows = ids_ref.shape[1]
    for row in range(rows):
        here = ids_ref[0, row]
        place = slice(row * cols, (row + 1) * cols)
        id_rows_ref[place, :] = jnp.full((cols, LANES), here, jnp.int32)
        for side, other in ((0, row - 1), (1, row + 1)):
            same = jnp.float32(0.0)
            if 0 <= other < rows:
                same = jnp.where(ids_ref[0, other] == here, 1.0, 0.0).astype(jnp.float32)
            mask_ref[side, place, :] = jnp.full((cols, LANES), same, jnp.float32)
    lane = lax.broadcasted_iota(jnp.int32, (8, LANES), 1)
    each = LANES // cols
    for block in range(rows // each):
        ids = jnp.full((8, LANES), ids_ref[0, block * each], jnp.int32)
        for step in range(1, each):
            ids = jnp.where(lane >= step * cols, ids_ref[0, block * each + step], ids)
        id_cols_ref[:, block * LANES : (block + 1) * LANES] = ids


def forward_kernel(
    height_ref,
    ids_ref,
    *refs,
    cols,
    score_scale,
    count,
):
    pieces, refs = refs[:count], refs[count:]
    (
        gains_hbm,
        shifts_hbm,
        biases_hbm,
        qv_bias_hbm,
        proj_bias_hbm,
        weights_hbm,
        qkv_hbm,
        proj_hbm,
        features_ref,
        act_one_ref,
        middle_ref,
        act_two_ref,
        residual_ref,
        normed_ref,
        table_ref,
        mask_ref,
        query_ref,
        key_ref,
        value_ref,
        soft_ref,
        out_flip_ref,
        output_ref,
        gains_ref,
        shifts_ref,
        biases_ref,
        qv_bias_ref,
        proj_bias_ref,
        weights_ref,
        qkv_ref,
        proj_ref,
        taps_ref,
        id_rows_ref,
        id_cols_ref,
        value_flip_ref,
        sems,
        piece_sems,
    ) = refs
    pixels, channels = features_ref.shape
    own_pixels = pixels // count
    height = height_ref[0]
    wide = jnp.float32
    arrivals = []
    for place in range(count):
        owner = height ^ place
        rows = pl.ds(pl.multiple_of(owner * own_pixels, own_pixels), own_pixels)
        arrivals.append(
            pltpu.make_async_copy(pieces[place], features_ref.at[rows, :], piece_sems.at[place])
        )
    moves = [
        (gains_hbm, gains_ref),
        (shifts_hbm, shifts_ref),
        (weights_hbm.at[0], weights_ref.at[0]),
        (biases_hbm, biases_ref),
        (weights_hbm.at[1], weights_ref.at[1]),
        (qkv_hbm, qkv_ref),
        (qv_bias_hbm, qv_bias_ref),
        (proj_hbm, proj_ref),
        (proj_bias_hbm, proj_bias_ref),
    ]
    copies = [
        pltpu.make_async_copy(source, target, sems.at[index])
        for index, (source, target) in enumerate(moves)
    ]
    for copy in arrivals + copies:
        copy.start()
    build_masks(ids_ref, mask_ref, id_rows_ref, id_cols_ref, cols)
    clear_edges(taps_ref, cols)
    for copy in arrivals:
        copy.wait()

    def read_input(rows):
        return features_ref[rows, :].astype(wide)

    def read_middle(rows):
        return middle_ref[rows, :]

    def read_residual(rows):
        return residual_ref[rows, :]

    table_ref[0:1, :], table_ref[1:2, :] = norm_stats(read_input, pixels, channels)
    copies[0].wait()
    copies[1].wait()
    table_ref[6:9, :] = gains_ref[...]
    table_ref[9:12, :] = shifts_ref[...]
    activate(read_input, *norm_rows(table_ref, 0), act_one_ref, taps_ref, cols)
    copies[2].wait()
    copies[3].wait()
    run_conv(
        taps_ref,
        product_forward(weights_ref.at[0]),
        mask_ref,
        middle_ref,
        lambda rows: biases_ref[0:1, :],
        cols,
    )
    table_ref[2:3, :], table_ref[3:4, :] = norm_stats(read_middle, pixels, channels)
    activate(read_middle, *norm_rows(table_ref, 1), act_two_ref, taps_ref, cols)
    copies[4].wait()
    run_conv(
        taps_ref,
        product_forward(weights_ref.at[1]),
        mask_ref,
        residual_ref,
        lambda rows: read_input(rows) + biases_ref[1:2, :],
        cols,
    )
    table_ref[4:5, :], table_ref[5:6, :] = norm_stats(read_residual, pixels, channels)
    mean, inverse, gain, shift = norm_rows(table_ref, 2)
    scale = inverse * gain
    for copy in copies[5:]:
        copy.wait()
    block = min(QUERY_ROWS, pixels)

    def project(index, carry):
        rows = pl.ds(pl.multiple_of(index * block, block), block)
        normed = ((residual_ref[rows, :] - mean) * scale + shift).astype(jnp.bfloat16)
        normed_ref[rows, :] = normed
        query_ref[rows, :] = (
            jnp.dot(normed, qkv_ref[:, 0:channels], preferred_element_type=wide)
            + qv_bias_ref[0:1, :]
        ).astype(jnp.bfloat16)
        key_ref[rows, :] = jnp.dot(
            normed, qkv_ref[:, channels : 2 * channels], preferred_element_type=wide
        ).astype(jnp.bfloat16)
        values = (
            jnp.dot(normed, qkv_ref[:, 2 * channels :], preferred_element_type=wide)
            + qv_bias_ref[1:2, :]
        ).astype(jnp.bfloat16)
        value_ref[rows, :] = values
        value_flip_ref[:, rows] = values.T
        return carry

    lax.fori_loop(0, pixels // block, project, 0)

    def attend(index, carry):
        rows = pl.ds(pl.multiple_of(index * block, block), block)
        scores = lax.dot_general(
            key_ref[...], query_ref[rows, :], (((1,), (1,)), ((), ())), preferred_element_type=wide
        )
        same = widen(id_rows_ref[...], block) == id_cols_ref[0:1, rows]
        scores = jnp.where(same, scores * score_scale, masked_score)
        scores = jnp.exp(scores - jnp.max(scores, axis=0, keepdims=True))
        weights = scores * (1.0 / jnp.sum(scores, axis=0, keepdims=True))
        soft_ref[:, rows] = weights
        out_flip_ref[:, rows] = jnp.dot(
            value_flip_ref[...], weights.astype(jnp.bfloat16), preferred_element_type=wide
        ).astype(jnp.bfloat16)
        return carry

    lax.fori_loop(0, pixels // block, attend, 0)
    own = pl.ds(pl.multiple_of(height * own_pixels, own_pixels), own_pixels)
    output_ref[...] = (
        residual_ref[own, :]
        + lax.dot_general(
            out_flip_ref[:, own],
            proj_ref[...],
            (((0,), (0,)), ((), ())),
            preferred_element_type=wide,
        )
        + proj_bias_ref[...]
    ).astype(jnp.bfloat16)


def attention_kernel(
    height_ref,
    grad_hbm,
    proj_hbm,
    normed_ref,
    query_ref,
    key_ref,
    value_ref,
    soft_ref,
    out_flip_ref,
    packed_ref,
    mixed_ref,
    sums_ref,
    grad_ref,
    proj_ref,
    key_flip_ref,
    key_sum_ref,
    value_sum_ref,
    flip_ref,
    sems,
    *,
    score_scale,
):
    pixels, channels = normed_ref.shape
    block = min(QUERY_ROWS, pixels)
    wide = jnp.float32
    copies = [
        pltpu.make_async_copy(grad_hbm, grad_ref, sems.at[0]),
        pltpu.make_async_copy(proj_hbm, proj_ref, sems.at[1]),
    ]
    for copy in copies:
        copy.start()
    half = channels // 2
    core = height_ref[0] & 1
    half_lanes = pl.ds(pl.multiple_of(core * half, half), half)
    flip_ref[...] = normed_ref[:, half_lanes].T
    key_flip_ref[...] = key_ref[...].T
    key_sum_ref[...] = jnp.zeros(key_sum_ref.shape, wide)
    value_sum_ref[...] = jnp.zeros(value_sum_ref.shape, wide)
    for copy in copies:
        copy.wait()

    def attend(index, carry):
        rows = pl.ds(pl.multiple_of(index * block, block), block)
        back = lax.dot_general(
            grad_ref[rows, :], proj_ref[...], (((1,), (1,)), ((), ())), preferred_element_type=wide
        ).astype(jnp.bfloat16)
        weights = soft_ref[:, rows]
        weight_grad = lax.dot_general(
            value_ref[...], back, (((1,), (1,)), ((), ())), preferred_element_type=wide
        )
        value_sum_ref[...] += jnp.dot(
            weights.astype(jnp.bfloat16), back, preferred_element_type=wide
        )
        dots = jnp.sum(weights * weight_grad, axis=0, keepdims=True)
        score_grad = (weights * (weight_grad - dots)).astype(jnp.bfloat16)
        key_sum_ref[...] += jnp.dot(score_grad, query_ref[rows, :], preferred_element_type=wide)
        query_grad = jnp.dot(key_flip_ref[...], score_grad, preferred_element_type=wide)
        packed_ref[rows, 0:channels] = (query_grad * score_scale).astype(jnp.bfloat16).T
        return carry

    lax.fori_loop(0, pixels // block, attend, 0)

    def pack(rows, carry):
        packed_ref[rows, channels : 2 * channels] = (key_sum_ref[rows, :] * score_scale).astype(
            jnp.bfloat16
        )
        packed_ref[rows, 2 * channels :] = value_sum_ref[rows, :].astype(jnp.bfloat16)
        return (
            carry[0] + fold(packed_ref[rows, 0:channels].astype(wide)),
            carry[1] + fold(packed_ref[rows, 2 * channels :].astype(wide)),
            carry[2] + fold(grad_ref[rows, :].astype(wide)),
        )

    zeros = jnp.zeros((8, channels), wide)
    totals = each_chunk(pixels, pack, (zeros, zeros, zeros))
    for row, total in enumerate(totals):
        sums_ref[row : row + 1, :] = column_total(total)

    share = mixed_ref.shape[1]
    part = jnp.dot(flip_ref[...], packed_ref[...], preferred_element_type=wide)
    half_rows = pl.ds(pl.multiple_of(core * half, half), half)
    proj_part = jnp.dot(out_flip_ref[half_rows, :], grad_ref[...], preferred_element_type=wide)
    for piece in range(mixed_ref.shape[0]):
        rows = slice(piece * share, (piece + 1) * share)
        mixed_ref[piece, :, 0 : 3 * channels] = part[rows].astype(jnp.bfloat16)
        mixed_ref[piece, :, 3 * channels :] = proj_part[rows].astype(jnp.bfloat16)


def third_kernel(
    height_ref,
    grad_hbm,
    qkv_hbm,
    packed_ref,
    residual_ref,
    table_ref,
    act_two_ref,
    mask_ref,
    residual_grad_ref,
    grad_two_ref,
    part_ref,
    sums_ref,
    grad_ref,
    qkv_ref,
    total_ref,
    narrow_ref,
    columns_ref,
    sems,
    *,
    cols,
):
    pixels, channels = residual_ref.shape
    block = min(CONV_ROWS, pixels)
    wide = jnp.float32
    copies = [
        pltpu.make_async_copy(qkv_hbm, qkv_ref, sems.at[0]),
        pltpu.make_async_copy(grad_hbm, grad_ref, sems.at[1]),
    ]
    for copy in copies:
        copy.start()
    mean, inverse, gain, shift = norm_rows(table_ref, 2)
    zeros = jnp.zeros((8, channels), wide)
    copies[0].wait()

    def input_grads(index, carry):
        rows = pl.ds(pl.multiple_of(index * block, block), block)
        normed_grad = lax.dot_general(
            packed_ref[rows, :], qkv_ref[...], (((1,), (1,)), ((), ())), preferred_element_type=wide
        )
        total_ref[rows, :] = normed_grad
        normed = (residual_ref[rows, :] - mean) * inverse
        return carry[0] + fold(normed_grad), carry[1] + fold(normed_grad * normed)

    sums = lax.fori_loop(0, pixels // block, input_grads, (zeros, zeros))
    sums_ref[0:1, :] = column_total(sums[1])
    sums_ref[1:2, :] = column_total(sums[0])
    mean_grad, mean_cross = back_means(sums, gain, pixels)
    copies[1].wait()

    def finish(rows, carry):
        normed = (residual_ref[rows, :] - mean) * inverse
        back = inverse * (total_ref[rows, :] * gain - mean_grad - normed * mean_cross)
        total = grad_ref[rows, :].astype(wide) + back
        residual_grad_ref[rows, :] = total
        low = total.astype(jnp.bfloat16)
        grad_two_ref[rows, :] = low
        return carry + fold(low.astype(wide))

    sums_ref[2:3, :] = column_total(each_chunk(pixels, finish, zeros))
    weight_part(
        height_ref[0], act_two_ref, grad_two_ref, mask_ref, narrow_ref, columns_ref, part_ref, cols
    )


def second_kernel(
    height_ref,
    grad_two_ref,
    middle_ref,
    table_ref,
    act_one_ref,
    mask_ref,
    weights_hbm,
    grad_one_ref,
    part_ref,
    sums_ref,
    weights_ref,
    taps_ref,
    total_ref,
    narrow_ref,
    columns_ref,
    sem,
    *,
    cols,
):
    pixels, channels = middle_ref.shape
    copy = pltpu.make_async_copy(weights_hbm.at[1], weights_ref, sem)
    copy.start()
    sums, back = conv_back(
        grad_two_ref,
        copy,
        weights_ref,
        mask_ref,
        taps_ref,
        total_ref,
        lambda rows: middle_ref[rows, :],
        table_ref,
        1,
        cols,
    )
    sums_ref[0:1, :] = column_total(sums[1])
    sums_ref[1:2, :] = column_total(sums[0])

    def finish(rows, carry):
        low = back(rows).astype(jnp.bfloat16)
        grad_one_ref[rows, :] = low
        return carry + fold(low.astype(jnp.float32))

    zeros = jnp.zeros((8, channels), jnp.float32)
    sums_ref[2:3, :] = column_total(each_chunk(pixels, finish, zeros))
    weight_part(
        height_ref[0], act_one_ref, grad_one_ref, mask_ref, narrow_ref, columns_ref, part_ref, cols
    )


def first_kernel(
    height_ref,
    grad_one_ref,
    features_ref,
    residual_grad_ref,
    table_ref,
    mask_ref,
    weights_hbm,
    input_grad_ref,
    sums_ref,
    weights_ref,
    taps_ref,
    total_ref,
    sem,
    *,
    cols,
):
    copy = pltpu.make_async_copy(weights_hbm.at[0], weights_ref, sem)
    copy.start()
    sums, back = conv_back(
        grad_one_ref,
        copy,
        weights_ref,
        mask_ref,
        taps_ref,
        total_ref,
        lambda rows: features_ref[rows, :].astype(jnp.float32),
        table_ref,
        0,
        cols,
    )
    sums_ref[0:1, :] = column_total(sums[1])
    sums_ref[1:2, :] = column_total(sums[0])
    count = input_grad_ref.shape[0]
    own = pl.ds(pl.multiple_of(height_ref[0] * count, count), count)
    input_grad_ref[...] = (residual_grad_ref[own, :] + back(own)).astype(jnp.bfloat16)


def join_kernel(
    height_ref,
    same_ref,
    other_ref,
    ones_ref,
    twos_ref,
    qkv_hbm,
    proj_hbm,
    conv_ref,
    qkv_ref,
    proj_ref,
    sems,
):
    half = same_ref.shape[0]
    inner = qkv_ref.shape[2]
    core = height_ref[0] & 1
    copies = []
    for index, (source, owner) in enumerate(((same_ref, core), (other_ref, 1 - core))):
        rows = pl.ds(pl.multiple_of(owner * half, half), half)
        qkv_ref[index] = source[:, 0:inner].astype(jnp.float32)
        proj_ref[index] = source[:, inner:].astype(jnp.float32)
        for which, (held, target) in enumerate(((qkv_ref, qkv_hbm), (proj_ref, proj_hbm))):
            copy = pltpu.make_async_copy(
                held.at[index], target.at[rows, :], sems.at[index, which]
            )
            copy.start()
            copies.append(copy)
    for which, parts_ref in enumerate((ones_ref, twos_ref)):
        total = parts_ref[0].astype(jnp.float32)
        for piece in range(1, parts_ref.shape[0]):
            total = total + parts_ref[piece].astype(jnp.float32)
        conv_ref[which] = total.reshape(conv_ref.shape[1:])
    for copy in copies:
        copy.wait()


def sums_kernel(*refs):
    gains_ref, shifts_ref, conv_ref, qv_ref, proj_ref = refs[-5:]
    total = refs[0][...]
    for ref in refs[1:-5]:
        total = total + ref[...]
    one, two, three, soft = 0, 8, 16, 24
    for row, start in enumerate((one, two, three)):
        gains_ref[row : row + 1, :] = total[start : start + 1]
        shifts_ref[row : row + 1, :] = total[start + 1 : start + 2]
    conv_ref[0:1, :] = total[two + 2 : two + 3]
    conv_ref[1:2, :] = total[three + 2 : three + 3]
    qv_ref[...] = total[soft : soft + 2]
    proj_ref[...] = total[soft + 2 : soft + 3]


def call_kernel(kernel, outputs, scratch, operands, places, flops, limit, out_places=None):
    spaces = {
        "v": pl.BlockSpec(memory_space=pltpu.VMEM),
        "s": pl.BlockSpec(memory_space=pltpu.SMEM),
        "h": pl.BlockSpec(memory_space=pl.ANY),
    }
    moved = sum(array.size * array.dtype.itemsize for array in operands)
    return pl.pallas_call(
        kernel,
        out_shape=[jax.ShapeDtypeStruct(shape, dtype) for shape, dtype in outputs],
        in_specs=[spaces[place] for place in places],
        out_specs=[spaces[place] for place in out_places or "v" * len(outputs)],
        scratch_shapes=scratch,
        compiler_params=pltpu.CompilerParams(vmem_limit_bytes=limit * 2**20),
        cost_estimate=pl.CostEstimate(flops=flops, bytes_accessed=moved, transcendentals=0),
    )(*operands)


def gather_height(block, size):
    held = [block] + [
        lax.ppermute(block, "height", [(i, i ^ step) for i in range(size)])
        for step in range(2, size, 2)
    ]
    pieces = []
    for piece in held:
        pieces.append(piece)
        pieces.append(lax.ppermute(piece, "height", [(i, i ^ 1) for i in range(size)]))
    return pieces


def whole_canvas(
    features,
    tile_ids,
    norm_gains,
    norm_shifts,
    conv_weights,
    conv_biases,
    qkv_weight,
    qv_bias,
    proj_weight,
    proj_bias,
    cotangent,
):
    height_size = lax.axis_size("height")
    canvas_size = lax.axis_size("canvas")
    local_rows, cols, channels = features.shape[1:]
    all_rows = tile_ids.shape[1]
    pixels = all_rows * cols
    own_pixels = local_rows * cols
    out_share = channels // height_size
    ci_share = channels // canvas_size
    row_share = channels // 2 // canvas_size
    low, wide = jnp.bfloat16, jnp.float32
    height = lax.axis_index("height").astype(jnp.int32).reshape(1)

    pieces = gather_height(features.reshape(own_pixels, channels), height_size)
    late_cotangent, *pieces = lax.optimization_barrier((cotangent[0], *pieces))
    out_grad = lax.all_gather(late_cotangent, "height", axis=0, tiled=True)
    out_grad = out_grad.reshape(pixels, channels)

    plane = ((pixels, channels), low)
    plane_wide = ((pixels, channels), wide)
    rows_wide = ((8, channels), wide)
    part_shape = ((canvas_size, 9 * out_share, ci_share), low)
    taps = pltpu.VMEM((pixels + 2 * cols, 3 * channels), low)
    held = pltpu.VMEM((pixels, channels), low)
    held_wide = pltpu.VMEM((pixels, channels), wide)
    flipped = pltpu.VMEM((channels, pixels), low)
    conv_held = pltpu.VMEM(conv_weights.shape[1:], low)
    narrow = pltpu.VMEM((pixels + 2 * cols, 3 * NARROW), wide)
    columns = pltpu.VMEM((pixels, 5 * NARROW), low)
    sem = pltpu.SemaphoreType.DMA
    conv_flops = 2 * 9 * pixels * channels * channels
    dot_flops = 2 * pixels * channels * channels
    score_flops = 2 * pixels * pixels * channels
    scale = channels ** (-0.5)

    (
        all_features,
        act_one,
        middle,
        act_two,
        residual,
        normed,
        table,
        mask,
        query,
        key,
        value,
        soft,
        out_flip,
        output,
    ) = call_kernel(
        functools.partial(forward_kernel, cols=cols, score_scale=scale, count=height_size),
        [
            plane,
            plane,
            plane_wide,
            plane,
            plane_wide,
            plane,
            ((16, channels), wide),
            ((2, pixels, LANES), wide),
            plane,
            plane,
            plane,
            ((pixels, pixels), wide),
            ((channels, pixels), low),
            ((own_pixels, channels), low),
        ],
        [
            pltpu.VMEM(norm_gains.shape, wide),
            pltpu.VMEM(norm_shifts.shape, wide),
            pltpu.VMEM(conv_biases.shape, wide),
            pltpu.VMEM(qv_bias.shape, wide),
            pltpu.VMEM((1, channels), wide),
            pltpu.VMEM(conv_weights.shape, low),
            pltpu.VMEM(qkv_weight.shape, low),
            pltpu.VMEM(proj_weight.shape, low),
            taps,
            pltpu.VMEM((pixels, LANES), jnp.int32),
            pltpu.VMEM((8, pixels), jnp.int32),
            flipped,
            sem((9,)),
            sem((height_size,)),
        ],
        [
            height,
            tile_ids,
            *pieces,
            norm_gains,
            norm_shifts,
            conv_biases,
            qv_bias,
            proj_bias.reshape(1, channels),
            conv_weights,
            qkv_weight,
            proj_weight,
        ],
        "ss" + "h" * (height_size + 8),
        2 * conv_flops + 3 * dot_flops + 2 * score_flops,
        40,
    )
    packed, mixed, sums_soft = call_kernel(
        functools.partial(attention_kernel, score_scale=scale),
        [
            ((pixels, 3 * channels), low),
            ((canvas_size, row_share, 4 * channels), low),
            rows_wide,
        ],
        [
            held,
            pltpu.VMEM(proj_weight.shape, low),
            flipped,
            held_wide,
            held_wide,
            pltpu.VMEM((channels // 2, pixels), low),
            sem((2,)),
        ],
        [height, out_grad, proj_weight, normed, query, key, value, soft, out_flip],
        "shhvvvvvv",
        3 * dot_flops + 4 * score_flops,
        32,
    )
    mixed_parts = lax.all_to_all(mixed, "canvas", 0, 0)
    residual_grad, grad_two, part_two, sums_three = call_kernel(
        functools.partial(third_kernel, cols=cols),
        [plane_wide, plane, part_shape, rows_wide],
        [held, pltpu.VMEM(qkv_weight.shape, low), held_wide, narrow, columns, sem((2,))],
        [height, out_grad, qkv_weight, packed, residual, table, act_two, mask],
        "shhvvvvv",
        3 * dot_flops + conv_flops // height_size,
        32,
    )
    parts_two = lax.all_to_all(part_two, "canvas", 0, 0)
    mixed_half = jnp.sum(mixed_parts.astype(wide), axis=0).astype(low)
    mixed_half = lax.all_gather(mixed_half, "canvas", axis=0, tiled=True)
    back_scratch = [conv_held, taps, held_wide]
    grad_one, part_one, sums_two = call_kernel(
        functools.partial(second_kernel, cols=cols),
        [plane, part_shape, rows_wide],
        back_scratch + [narrow, columns, sem],
        [height, grad_two, middle, table, act_one, mask, conv_weights],
        "svvvvvh",
        conv_flops + conv_flops // height_size,
        32,
    )
    parts_one = lax.all_to_all(part_one, "canvas", 0, 0)
    mixed_other = lax.ppermute(mixed_half, "height", [(i, i ^ 1) for i in range(height_size)])
    input_grad, sums_one = call_kernel(
        functools.partial(first_kernel, cols=cols),
        [((own_pixels, channels), low), rows_wide],
        back_scratch + [sem],
        [height, grad_one, all_features, residual_grad, table, mask, conv_weights],
        "svvvvvh",
        conv_flops,
        32,
    )
    sums = jnp.concatenate([sums_one, sums_two, sums_three, sums_soft], axis=0)
    all_sums = [sums] + [
        lax.ppermute(sums, "canvas", [(i, i ^ step) for i in range(canvas_size)])
        for step in range(1, canvas_size)
    ]
    qkv_grad, proj_grad, conv_grad = call_kernel(
        join_kernel,
        [
            (qkv_weight.shape, wide),
            (proj_weight.shape, wide),
            ((2, 3, 3, out_share, ci_share), wide),
        ],
        [
            pltpu.VMEM((2, channels // 2, 3 * channels), wide),
            pltpu.VMEM((2, channels // 2, channels), wide),
            sem((2, 2)),
        ],
        [height, mixed_half, mixed_other, parts_one, parts_two],
        "svvvv",
        0,
        32,
        "hhv",
    )
    vector_shapes = [norm_gains.shape, norm_shifts.shape, conv_biases.shape, qv_bias.shape]
    gains_grad, shifts_grad, biases_grad, qv_grad, proj_bias_grad = call_kernel(
        sums_kernel,
        [(shape, wide) for shape in vector_shapes + [(1, channels)]],
        [],
        all_sums,
        "v" * canvas_size,
        0,
        16,
    )
    own_shape = (1, local_rows, cols, channels)
    return (
        output.reshape(own_shape),
        input_grad.reshape(own_shape),
        gains_grad,
        shifts_grad,
        jnp.swapaxes(conv_grad, 3, 4),
        biases_grad,
        qkv_grad,
        qv_grad,
        proj_grad,
        proj_bias_grad.reshape(channels),
    )


def on_device(*arrays):
    features, tile_ids = arrays[0], arrays[1]
    local_rows, cols, channels = features.shape[1:]
    pixels = tile_ids.shape[1] * cols
    height_size, canvas_size = lax.axis_size("height"), lax.axis_size("canvas")
    powers = all(size & (size - 1) == 0 for size in (height_size, canvas_size, cols))
    fits = (
        powers
        and height_size > 1
        and pixels <= MOST_PIXELS
        and pixels % CONV_ROWS == 0
        and (local_rows * cols) % LANES == 0
        and CHUNK % cols == 0
        and cols % 16 == 0
        and channels % (LANES * canvas_size) == 0
        and 2 * channels == NARROW * height_size
    )
    return whole_canvas(*arrays) if fits else split_canvas(*arrays)


def solution(mesh):
    in_specs = (
        P("canvas", "height", None, None),
        P("canvas", None),
        P(),
        P(),
        P(),
        P(),
        P(),
        P(),
        P(),
        P(),
        P("canvas", "height", None, None),
    )
    out_specs = (
        P("canvas", "height", None, None),
        P("canvas", "height", None, None),
        P(),
        P(),
        P(None, None, None, "canvas", "height"),
        P(),
        P(),
        P(),
        P(),
        P(),
    )
    return jax.shard_map(
        on_device, mesh=mesh, in_specs=in_specs, out_specs=out_specs, check_vma=False
    )
```

```python
import functools

import jax
import jax.numpy as jnp
from jax import lax
from jax.experimental import pallas as pl
from jax.experimental.pallas import tpu as pltpu
from jax.sharding import PartitionSpec as P

GROUPS = 32


epsilon = 1e-06
masked_score = -1e30
MOST_PIXELS = 1024
LANES = 128
NARROW = 128
CHUNK = 128
CONV_ROWS = 512
QUERY_ROWS = 256


def extended(block, sides, width):
    for axis, dim in sides:
        count = lax.axis_size(axis)
        forward = [(i, i + 1) for i in range(count - 1)]
        backward = [(target, source) for source, target in forward]
        low = lax.ppermute(
            lax.slice_in_dim(block, block.shape[dim] - width, None, axis=dim), axis, forward
        )
        high = lax.ppermute(lax.slice_in_dim(block, 0, width, axis=dim), axis, backward)
        block = jnp.concatenate([low, block, high], axis=dim)
    return block


def group_total(vector):
    return vector.reshape(GROUPS, -1).sum(axis=1)


def spread_groups(vector, channels):
    return jnp.repeat(vector, channels // GROUPS)


def norm_forward(values, gain, shift, members):
    channels = values.shape[1]
    totals = lax.psum(group_total(jnp.sum(values, axis=0)), "height")
    centered = values - spread_groups(totals / members, channels)
    squares = lax.psum(group_total(jnp.sum(centered * centered, axis=0)), "height")
    inverse = spread_groups(lax.rsqrt(squares / members + epsilon), channels)
    normed = centered * inverse
    return (normed, inverse, normed * gain + shift)


def norm_backward(grad_in, normed, inverse, gain, members):
    channels = grad_in.shape[1]
    scaled = grad_in * gain
    both_sums = lax.psum(
        (group_total(jnp.sum(scaled, axis=0)), group_total(jnp.sum(scaled * normed, axis=0))),
        "height",
    )
    mean_grad = spread_groups(both_sums[0] / members, channels)
    mean_cross = spread_groups(both_sums[1] / members, channels)
    result = inverse * (scaled - mean_grad - normed * mean_cross)
    return (result, jnp.sum(grad_in * normed, axis=0), jnp.sum(grad_in, axis=0))


def swish(values):
    return values * jax.nn.sigmoid(values)


def swish_slope(values):
    sigmoid_part = jax.nn.sigmoid(values)
    return sigmoid_part * (1.0 + values * (1.0 - sigmoid_part))


def tap_columns(padded, row_mask, local_rows, canvas_cols):
    pieces = []
    for row_tap in range(3):
        rows_taken = padded[row_tap : row_tap + local_rows] * row_mask[:, row_tap, None, None]
        for col_tap in range(3):
            pieces.append(rows_taken[:, col_tap : col_tap + canvas_cols])
    stacked = jnp.concatenate(pieces, axis=2)
    return stacked.reshape(local_rows * canvas_cols, stacked.shape[2])


def conv_forward(acts, row_mask, weight, bias):
    local_rows, canvas_cols, channels = acts.shape
    rimmed = extended(acts, (("height", 0),), 1)
    padded = jnp.pad(rimmed, ((0, 0), (1, 1), (0, 0)))
    gathered = tap_columns(padded, row_mask, local_rows, canvas_cols)
    result = (
        jnp.dot(
            gathered, weight.reshape(9 * channels, channels), preferred_element_type=jnp.float32
        )
        + bias
    )
    return (result, gathered)


def conv_backward(grad_low, row_mask, weight, gathered):
    local_rows, canvas_cols, channels = grad_low.shape
    flat_grad = grad_low.reshape(local_rows * canvas_cols, channels)
    weight_grad = lax.dot_general(
        gathered, flat_grad, (((0,), (0,)), ((), ())), preferred_element_type=jnp.float32
    )
    rimmed = extended(grad_low, (("height", 0),), 1)
    padded = jnp.pad(rimmed, ((0, 0), (1, 1), (0, 0)))
    grad_taps = tap_columns(padded, row_mask, local_rows, canvas_cols)
    flipped = jnp.transpose(weight[::-1, ::-1], (0, 1, 3, 2)).reshape(9 * channels, channels)
    input_part = jnp.dot(grad_taps, flipped, preferred_element_type=jnp.float32)
    return (
        input_part,
        weight_grad.reshape(3, 3, channels, channels),
        jnp.sum(flat_grad.astype(jnp.float32), axis=0),
    )


def take_rows(array, offset, count):
    return lax.dynamic_slice_in_dim(array, offset, count)


def score_grads(
    queries, out_grad, log_total, row_dots, query_ids, key_rows, value_rows, key_ids, score_scale
):
    scores = (
        lax.dot_general(
            queries, key_rows, (((1,), (1,)), ((), ())), preferred_element_type=jnp.float32
        )
        * score_scale
    )
    same_tile = query_ids[:, None] == key_ids[None, :]
    softmax_block = jnp.exp(jnp.where(same_tile, scores - log_total[:, None], masked_score))
    weight_grad = lax.dot_general(
        out_grad, value_rows, (((1,), (1,)), ((), ())), preferred_element_type=jnp.float32
    )
    score_grad = (softmax_block * (weight_grad - row_dots[:, None])).astype(jnp.bfloat16)
    return (softmax_block.astype(jnp.bfloat16), score_grad)


def split_canvas(
    features,
    tile_ids,
    norm_gains,
    norm_shifts,
    conv_weights,
    conv_biases,
    qkv_weight,
    qv_bias,
    proj_weight,
    proj_bias,
    cotangent,
):
    height_size = lax.axis_size("height")
    local_rows = features.shape[1]
    canvas_cols = features.shape[2]
    channels = features.shape[3]
    pixels = local_rows * canvas_cols
    row_ids = tile_ids[0]
    all_rows = row_ids.shape[0]
    members = float(all_rows * canvas_cols * (channels // GROUPS))
    score_scale = channels ** (-0.5)
    first_row = lax.axis_index("height") * local_rows
    edge_ids = jnp.full((1,), -1, jnp.int32)
    padded_ids = jnp.concatenate([edge_ids, row_ids, edge_ids])
    near_ids = lax.dynamic_slice_in_dim(padded_ids, first_row, local_rows + 2)
    own_rows = near_ids[1 : local_rows + 1]
    row_mask = jnp.stack(
        [near_ids[row_tap : row_tap + local_rows] == own_rows for row_tap in range(3)], axis=1
    ).astype(jnp.bfloat16)
    key_ids = jnp.repeat(row_ids, canvas_cols)
    query_ids = jnp.repeat(own_rows, canvas_cols)
    grid_shape = (local_rows, canvas_cols, channels)
    inputs = features[0].reshape(pixels, channels).astype(jnp.float32)
    normed_one, inverse_one, pre_one = norm_forward(inputs, norm_gains[0], norm_shifts[0], members)
    act_one = swish(pre_one).astype(jnp.bfloat16).reshape(grid_shape)
    middle, taps_one = conv_forward(act_one, row_mask, conv_weights[0], conv_biases[0])
    normed_two, inverse_two, pre_two = norm_forward(middle, norm_gains[1], norm_shifts[1], members)
    act_two = swish(pre_two).astype(jnp.bfloat16).reshape(grid_shape)
    branch, taps_two = conv_forward(act_two, row_mask, conv_weights[1], conv_biases[1])
    residual = inputs + branch
    normed_three, inverse_three, pre_three = norm_forward(
        residual, norm_gains[2], norm_shifts[2], members
    )
    attn_input = pre_three.astype(jnp.bfloat16)
    mixed = jnp.dot(attn_input, qkv_weight, preferred_element_type=jnp.float32)
    queries = (mixed[:, :channels] + qv_bias[0]).astype(jnp.bfloat16)
    key_rows = mixed[:, channels : 2 * channels].astype(jnp.bfloat16)
    value_rows = (mixed[:, 2 * channels :] + qv_bias[1]).astype(jnp.bfloat16)
    running_max = jnp.full((pixels,), masked_score, jnp.float32)
    key_piece = lax.all_gather(key_rows, "height", axis=0, tiled=True)
    value_piece = lax.all_gather(value_rows, "height", axis=0, tiled=True)
    scores = (
        lax.dot_general(
            queries, key_piece, (((1,), (1,)), ((), ())), preferred_element_type=jnp.float32
        )
        * score_scale
    )
    same_tile = query_ids[:, None] == key_ids[None, :]
    scores = jnp.where(same_tile, scores, masked_score)
    new_max = jnp.maximum(running_max, jnp.max(scores, axis=1))
    weights = jnp.where(same_tile, jnp.exp(scores - new_max[:, None]), 0.0)
    summed_out = jnp.dot(
        weights.astype(jnp.bfloat16), value_piece, preferred_element_type=jnp.float32
    )
    total_weight = jnp.sum(weights, axis=1)
    log_total = new_max + jnp.log(total_weight)
    attended = summed_out / total_weight[:, None]
    attended_low = attended.astype(jnp.bfloat16)
    output = (
        residual
        + jnp.dot(attended_low, proj_weight, preferred_element_type=jnp.float32)
        + proj_bias
    )
    out_grad = cotangent[0].reshape(pixels, channels)
    out_grad_full = out_grad.astype(jnp.float32)
    proj_grad = lax.dot_general(
        attended_low, out_grad, (((0,), (0,)), ((), ())), preferred_element_type=jnp.float32
    )
    proj_bias_grad = jnp.sum(out_grad_full, axis=0)
    attended_grad = lax.dot_general(
        out_grad, proj_weight, (((1,), (1,)), ((), ())), preferred_element_type=jnp.float32
    ).astype(jnp.bfloat16)
    row_dots = jnp.sum(attended_grad.astype(jnp.float32) * attended, axis=1)
    block_rows = pixels * min(height_size, 8)
    zero_block = jnp.zeros((pixels, channels), jnp.float32)
    key_all, value_all = (
        lax.all_gather(key_rows, "height", axis=0, tiled=True),
        lax.all_gather(value_rows, "height", axis=0, tiled=True),
    )
    query_all, grad_all = (
        lax.all_gather(queries, "height", axis=0, tiled=True),
        lax.all_gather(attended_grad, "height", axis=0, tiled=True),
    )
    total_all, dots_all = (
        lax.all_gather(log_total, "height", axis=0, tiled=True),
        lax.all_gather(row_dots, "height", axis=0, tiled=True),
    )

    def own_query_step(running, block_index):
        offset = block_index * block_rows
        key_part = take_rows(key_all, offset, block_rows)
        rounded, score_grad = score_grads(
            queries,
            attended_grad,
            log_total,
            row_dots,
            query_ids,
            key_part,
            take_rows(value_all, offset, block_rows),
            take_rows(key_ids, offset, block_rows),
            score_scale,
        )
        return (
            running
            + jnp.dot(score_grad, key_part, preferred_element_type=jnp.float32) * score_scale,
            None,
        )

    def own_key_step(running, block_index):
        offset = block_index * block_rows
        query_part = take_rows(query_all, offset, block_rows)
        grad_part = take_rows(grad_all, offset, block_rows)
        rounded, score_grad = score_grads(
            query_part,
            grad_part,
            take_rows(total_all, offset, block_rows),
            take_rows(dots_all, offset, block_rows),
            take_rows(key_ids, offset, block_rows),
            key_rows,
            value_rows,
            query_ids,
            score_scale,
        )
        key_part = (
            lax.dot_general(
                score_grad, query_part, (((0,), (0,)), ((), ())), preferred_element_type=jnp.float32
            )
            * score_scale
        )
        value_part = lax.dot_general(
            rounded, grad_part, (((0,), (0,)), ((), ())), preferred_element_type=jnp.float32
        )
        return ((running[0] + key_part, running[1] + value_part), None)

    block_count = key_all.shape[0] // block_rows
    query_grad, unused_one = lax.scan(own_query_step, zero_block, jnp.arange(block_count))
    (key_grad, value_grad), unused_two = lax.scan(
        own_key_step, (zero_block, zero_block), jnp.arange(block_count)
    )
    query_low = query_grad.astype(jnp.bfloat16)
    key_low = key_grad.astype(jnp.bfloat16)
    value_low = value_grad.astype(jnp.bfloat16)
    stacked_grad = jnp.concatenate([query_low, key_low, value_low], axis=1)
    qkv_grad = lax.dot_general(
        attn_input, stacked_grad, (((0,), (0,)), ((), ())), preferred_element_type=jnp.float32
    )
    qv_grad = jnp.stack(
        [
            jnp.sum(query_low.astype(jnp.float32), axis=0),
            jnp.sum(value_low.astype(jnp.float32), axis=0),
        ]
    )
    normed_grad = lax.dot_general(
        stacked_grad, qkv_weight, (((1,), (1,)), ((), ())), preferred_element_type=jnp.float32
    )
    back_three, gain_three, shift_three = norm_backward(
        normed_grad, normed_three, inverse_three, norm_gains[2], members
    )
    residual_grad = out_grad_full + back_three
    grad_two = residual_grad.astype(jnp.bfloat16).reshape(grid_shape)
    act_two_grad, weight_two_grad, bias_two_grad = conv_backward(
        grad_two, row_mask, conv_weights[1], taps_two
    )
    middle_grad, gain_two, shift_two = norm_backward(
        act_two_grad * swish_slope(pre_two), normed_two, inverse_two, norm_gains[1], members
    )
    grad_one = middle_grad.astype(jnp.bfloat16).reshape(grid_shape)
    act_one_grad, weight_one_grad, bias_one_grad = conv_backward(
        grad_one, row_mask, conv_weights[0], taps_one
    )
    input_back, gain_one, shift_one = norm_backward(
        act_one_grad * swish_slope(pre_one), normed_one, inverse_one, norm_gains[0], members
    )
    input_grad = residual_grad + input_back
    conv_grad = jnp.stack([weight_one_grad, weight_two_grad])
    conv_part = lax.psum_scatter(conv_grad, "height", scatter_dimension=4, tiled=True)
    conv_part = lax.psum_scatter(
        conv_part.astype(jnp.bfloat16), "canvas", scatter_dimension=3, tiled=True
    ).astype(jnp.float32)
    summed = lax.psum(
        (
            jnp.stack([gain_one, gain_two, gain_three]),
            jnp.stack([shift_one, shift_two, shift_three]),
            jnp.stack([bias_one_grad, bias_two_grad]),
            qkv_grad,
            qv_grad,
            proj_grad,
            proj_bias_grad,
        ),
        ("canvas", "height"),
    )
    return (
        output.astype(jnp.bfloat16).reshape((1,) + grid_shape),
        input_grad.astype(jnp.bfloat16).reshape((1,) + grid_shape),
        summed[0],
        summed[1],
        conv_part,
        summed[2],
        summed[3],
        summed[4],
        summed[5],
        summed[6],
    )


def fold(block):
    rows, width = block.shape
    return jnp.sum(block.reshape(rows // 8, 8, width), axis=0)


def group_lanes(block, group):
    lane = lax.broadcasted_iota(jnp.int32, block.shape, 1)
    width = block.shape[1]
    step = 1
    while step < group:
        above = pltpu.roll(block, step, 1)
        below = pltpu.roll(block, width - step, 1)
        block = block + jnp.where((lane & step) != 0, above, below)
        step *= 2
    return block


def group_mean(partial, members):
    spread = group_lanes(partial, partial.shape[1] // GROUPS)
    return jnp.sum(spread, axis=0, keepdims=True) * (1.0 / members)


def widen(block, width):
    return jnp.concatenate([block] * (width // block.shape[1]), axis=1)


def each_chunk(pixels, body, carry):
    def step(index, carry):
        return body(pl.ds(pl.multiple_of(index * CHUNK, CHUNK), CHUNK), carry)

    return lax.fori_loop(0, pixels // CHUNK, step, carry)


def norm_stats(read, pixels, channels):
    members = float(pixels * (channels // GROUPS))
    zeros = jnp.zeros((8, channels), jnp.float32)
    total = each_chunk(pixels, lambda rows, carry: carry + fold(read(rows)), zeros)
    mean = group_mean(total, members)

    def squares(rows, carry):
        centered = read(rows) - mean
        return carry + fold(centered * centered)

    spread = group_mean(each_chunk(pixels, squares, zeros), members)
    return mean, lax.rsqrt(spread + epsilon)


def put_taps(taps_ref, block, rows, cols):
    count, channels = block.shape
    place = lax.broadcasted_iota(jnp.int32, block.shape, 0) & (cols - 1)
    left = jnp.where(place == 0, 0.0, pltpu.roll(block, 1, 0))
    right = jnp.where(place == cols - 1, 0.0, pltpu.roll(block, count - 1, 0))
    inner = pl.ds(pl.multiple_of(rows.start + cols, cols), count)
    taps_ref[inner, 0:channels] = left.astype(jnp.bfloat16)
    taps_ref[inner, channels : 2 * channels] = block.astype(jnp.bfloat16)
    taps_ref[inner, 2 * channels :] = right.astype(jnp.bfloat16)


def clear_edges(taps_ref, cols):
    edge = jnp.zeros((cols, taps_ref.shape[1]), taps_ref.dtype)
    taps_ref[0:cols, :] = edge
    taps_ref[taps_ref.shape[0] - cols :, :] = edge


def run_conv(taps_ref, product, mask_ref, total_ref, first, cols):
    pixels, channels = total_ref.shape
    block = min(CONV_ROWS, pixels)
    for row_tap in (1, 0, 2):

        def step(index, carry):
            start = pl.multiple_of(index * block, block)
            rows = pl.ds(start, block)
            shifted = pl.ds(pl.multiple_of(start + row_tap * cols, cols), block)
            part = product(taps_ref, shifted, row_tap)
            if row_tap == 1:
                total_ref[rows, :] = first(rows) + part
            else:
                total_ref[rows, :] += widen(mask_ref[row_tap // 2, rows, :], channels) * part
            return carry

        lax.fori_loop(0, pixels // block, step, 0)


def product_forward(weight_ref):
    channels = weight_ref.shape[-1]

    def product(taps_ref, shifted, row_tap):
        return jnp.dot(
            taps_ref[shifted, :],
            weight_ref[row_tap].reshape(3 * channels, channels),
            preferred_element_type=jnp.float32,
        )

    return product


def product_backward(weight_ref):
    channels = weight_ref.shape[-1]

    def product(taps_ref, shifted, row_tap):
        total = None
        for col_tap in range(3):
            part = lax.dot_general(
                taps_ref[shifted, col_tap * channels : (col_tap + 1) * channels],
                weight_ref[2 - row_tap, 2 - col_tap],
                (((1,), (1,)), ((), ())),
                preferred_element_type=jnp.float32,
            )
            total = part if total is None else total + part
        return total

    return product


def smooth(values):
    part = 0.5 * jnp.tanh(0.5 * values) + 0.5
    return values * part, part


def activate(read, mean, inverse, gain, shift, act_ref, taps_ref, cols):
    scale = inverse * gain

    def step(rows, carry):
        act = smooth((read(rows) - mean) * scale + shift)[0]
        act_ref[rows, :] = act.astype(jnp.bfloat16)
        put_taps(taps_ref, act, rows, cols)
        return carry

    each_chunk(act_ref.shape[0], step, 0)


def back_sums(read_pair, pixels, channels):
    zeros = jnp.zeros((8, channels), jnp.float32)

    def step(rows, carry):
        grad, normed = read_pair(rows)
        return carry[0] + fold(grad), carry[1] + fold(grad * normed)

    plain, cross = each_chunk(pixels, step, (zeros, zeros))
    return plain, cross


def back_means(sums, gain, pixels):
    channels = gain.shape[1]
    members = float(pixels * (channels // GROUPS))
    return group_mean(sums[0] * gain, members), group_mean(sums[1] * gain, members)


def column_total(partial):
    return jnp.sum(partial, axis=0, keepdims=True)


def weight_part(act_ref, grad_ref, mask_ref, narrow_ref, columns_ref, part_ref, out_refs, cols):
    pixels, channels = act_ref.shape
    height = lax.axis_index("height")
    share = NARROW // 2
    block = pl.ds(pl.multiple_of((height // 2) * NARROW, NARROW), NARROW)
    parity = height % 2
    edge = jnp.zeros((cols, 3 * NARROW), jnp.float32)
    narrow_ref[0:cols, :] = edge
    narrow_ref[cols + pixels :, :] = edge

    def spread(rows, carry):
        own = grad_ref[rows, block].astype(jnp.float32)
        half = lax.broadcasted_iota(jnp.int32, own.shape, 1) // share
        turned = pltpu.roll(own, share, 1)
        both = jnp.where(half == parity, own, turned)
        place = lax.broadcasted_iota(jnp.int32, own.shape, 0) & (cols - 1)
        left = jnp.where(place == 0, 0.0, pltpu.roll(both, 1, 0))
        right = jnp.where(place == cols - 1, 0.0, pltpu.roll(both, CHUNK - 1, 0))
        inner = pl.ds(pl.multiple_of(rows.start + cols, cols), CHUNK)
        narrow_ref[inner, 0:NARROW] = left
        narrow_ref[inner, NARROW : 2 * NARROW] = both
        narrow_ref[inner, 2 * NARROW :] = right
        return carry

    each_chunk(pixels, spread, 0)

    def gather(rows, carry):
        taps = []
        for row_tap in range(3):
            for col_tap in range(3):
                row_back, col_back = 2 - row_tap, 2 - col_tap
                shifted = pl.ds(pl.multiple_of(rows.start + row_back * cols, cols), CHUNK)
                block = narrow_ref[shifted, col_back * NARROW : (col_back + 1) * NARROW]
                if row_back != 1:
                    block = block * mask_ref[row_back // 2, rows, :]
                taps.append(block)
        lower = lax.broadcasted_iota(jnp.int32, taps[0].shape, 1) < share
        for pair in range(5):
            second = taps[min(2 * pair + 1, 8)]
            columns_ref[rows, pair * NARROW : (pair + 1) * NARROW] = jnp.where(
                lower, taps[2 * pair], second
            ).astype(jnp.bfloat16)
        return carry

    each_chunk(pixels, gather, 0)
    part_ref[...] = lax.dot_general(
        columns_ref[...],
        act_ref[...],
        (((0,), (0,)), ((), ())),
        preferred_element_type=jnp.float32,
    ).astype(jnp.bfloat16)
    rows, width = out_refs[0].shape
    send_order(part_ref.at[0:rows, :], out_refs, 1, width)


def conv_back(grad_ref, copy, weights_ref, mask_ref, taps_ref, total_ref, read, table_ref, which, cols):
    pixels, channels = total_ref.shape
    wide = jnp.float32
    clear_edges(taps_ref, cols)

    def spread(rows, carry):
        put_taps(taps_ref, grad_ref[rows, :].astype(wide), rows, cols)
        return carry

    each_chunk(pixels, spread, 0)
    copy.wait()
    run_conv(
        taps_ref, product_backward(weights_ref), mask_ref, total_ref, lambda rows: 0.0, cols
    )
    mean, inverse, gain, shift = norm_rows(table_ref, which)

    def slope(rows):
        normed = (read(rows) - mean) * inverse
        pre = normed * gain + shift
        part = smooth(pre)[1]
        grad = total_ref[rows, :] * (part * (1.0 + pre * (1.0 - part)))
        total_ref[rows, :] = grad
        return grad, normed

    sums = back_sums(slope, pixels, channels)
    mean_grad, mean_cross = back_means(sums, gain, pixels)

    def back(rows):
        normed = (read(rows) - mean) * inverse
        return inverse * (total_ref[rows, :] * gain - mean_grad - normed * mean_cross)

    return sums, back


def norm_rows(table_ref, which):
    picks = (2 * which, 2 * which + 1, 6 + which, 9 + which)
    return tuple(table_ref[pick : pick + 1, :] for pick in picks)


def build_masks(ids_ref, mask_ref, id_rows_ref, id_cols_ref, cols):
    rows = ids_ref.shape[1]
    for row in range(rows):
        here = ids_ref[0, row]
        place = slice(row * cols, (row + 1) * cols)
        id_rows_ref[place, :] = jnp.full((cols, LANES), here, jnp.int32)
        for side, other in ((0, row - 1), (1, row + 1)):
            same = jnp.float32(0.0)
            if 0 <= other < rows:
                same = jnp.where(ids_ref[0, other] == here, 1.0, 0.0).astype(jnp.float32)
            mask_ref[side, place, :] = jnp.full((cols, LANES), same, jnp.float32)
    lane = lax.broadcasted_iota(jnp.int32, (8, LANES), 1)
    each = LANES // cols
    for block in range(rows // each):
        ids = jnp.full((8, LANES), ids_ref[0, block * each], jnp.int32)
        for step in range(1, each):
            ids = jnp.where(lane >= step * cols, ids_ref[0, block * each + step], ids)
        id_cols_ref[:, block * LANES : (block + 1) * LANES] = ids


def forward_kernel(
    *refs,
    cols,
    score_scale,
    count,
):
    pieces, refs = refs[:count], refs[count:]
    (
        ids_hbm,
        gains_hbm,
        shifts_hbm,
        biases_hbm,
        qv_bias_hbm,
        proj_bias_hbm,
        weights_hbm,
        qkv_hbm,
        proj_hbm,
        features_ref,
        act_one_ref,
        middle_ref,
        act_two_ref,
        residual_ref,
        normed_ref,
        table_ref,
        mask_ref,
        query_ref,
        key_ref,
        value_ref,
        soft_ref,
        out_flip_ref,
        output_ref,
        ids_ref,
        gains_ref,
        shifts_ref,
        biases_ref,
        qv_bias_ref,
        proj_bias_ref,
        weights_ref,
        qkv_ref,
        proj_ref,
        taps_ref,
        id_rows_ref,
        id_cols_ref,
        value_flip_ref,
        sems,
        piece_sems,
    ) = refs
    pixels, channels = features_ref.shape
    own_pixels = pixels // count
    height = lax.axis_index("height")
    wide = jnp.float32
    arrivals = []
    for place in range(count):
        owner = height ^ place
        rows = pl.ds(pl.multiple_of(owner * own_pixels, own_pixels), own_pixels)
        arrivals.append(
            pltpu.make_async_copy(pieces[place], features_ref.at[rows, :], piece_sems.at[place])
        )
    moves = [
        (gains_hbm, gains_ref),
        (shifts_hbm, shifts_ref),
        (weights_hbm.at[0], weights_ref.at[0]),
        (biases_hbm, biases_ref),
        (weights_hbm.at[1], weights_ref.at[1]),
        (qkv_hbm, qkv_ref),
        (qv_bias_hbm, qv_bias_ref),
        (proj_hbm, proj_ref),
        (proj_bias_hbm, proj_bias_ref),
        (ids_hbm, ids_ref),
    ]
    copies = [
        pltpu.make_async_copy(source, target, sems.at[index])
        for index, (source, target) in enumerate(moves)
    ]
    for copy in [copies[-1]] + arrivals + copies[:-1]:
        copy.start()
    copies[-1].wait()
    build_masks(ids_ref, mask_ref, id_rows_ref, id_cols_ref, cols)
    clear_edges(taps_ref, cols)
    for copy in arrivals:
        copy.wait()

    def read_input(rows):
        return features_ref[rows, :].astype(wide)

    def read_middle(rows):
        return middle_ref[rows, :]

    def read_residual(rows):
        return residual_ref[rows, :]

    table_ref[0:1, :], table_ref[1:2, :] = norm_stats(read_input, pixels, channels)
    copies[0].wait()
    copies[1].wait()
    table_ref[6:9, :] = gains_ref[...]
    table_ref[9:12, :] = shifts_ref[...]
    activate(read_input, *norm_rows(table_ref, 0), act_one_ref, taps_ref, cols)
    copies[2].wait()
    copies[3].wait()
    run_conv(
        taps_ref,
        product_forward(weights_ref.at[0]),
        mask_ref,
        middle_ref,
        lambda rows: biases_ref[0:1, :],
        cols,
    )
    table_ref[2:3, :], table_ref[3:4, :] = norm_stats(read_middle, pixels, channels)
    activate(read_middle, *norm_rows(table_ref, 1), act_two_ref, taps_ref, cols)
    copies[4].wait()
    run_conv(
        taps_ref,
        product_forward(weights_ref.at[1]),
        mask_ref,
        residual_ref,
        lambda rows: read_input(rows) + biases_ref[1:2, :],
        cols,
    )
    table_ref[4:5, :], table_ref[5:6, :] = norm_stats(read_residual, pixels, channels)
    mean, inverse, gain, shift = norm_rows(table_ref, 2)
    scale = inverse * gain
    for copy in copies[5:-1]:
        copy.wait()
    block = min(QUERY_ROWS, pixels)

    def project(index, carry):
        rows = pl.ds(pl.multiple_of(index * block, block), block)
        normed = ((residual_ref[rows, :] - mean) * scale + shift).astype(jnp.bfloat16)
        normed_ref[rows, :] = normed
        query_ref[rows, :] = (
            jnp.dot(normed, qkv_ref[:, 0:channels], preferred_element_type=wide)
            + qv_bias_ref[0:1, :]
        ).astype(jnp.bfloat16)
        key_ref[rows, :] = jnp.dot(
            normed, qkv_ref[:, channels : 2 * channels], preferred_element_type=wide
        ).astype(jnp.bfloat16)
        values = (
            jnp.dot(normed, qkv_ref[:, 2 * channels :], preferred_element_type=wide)
            + qv_bias_ref[1:2, :]
        ).astype(jnp.bfloat16)
        value_ref[rows, :] = values
        value_flip_ref[:, rows] = values.T
        return carry

    lax.fori_loop(0, pixels // block, project, 0)

    def attend(index, carry):
        rows = pl.ds(pl.multiple_of(index * block, block), block)
        scores = lax.dot_general(
            key_ref[...], query_ref[rows, :], (((1,), (1,)), ((), ())), preferred_element_type=wide
        )
        same = widen(id_rows_ref[...], block) == id_cols_ref[0:1, rows]
        scores = jnp.where(same, scores * score_scale, masked_score)
        scores = jnp.exp(scores - jnp.max(scores, axis=0, keepdims=True))
        weights = scores * (1.0 / jnp.sum(scores, axis=0, keepdims=True))
        rounded = weights.astype(jnp.bfloat16)
        soft_ref[:, rows] = rounded
        out_flip_ref[:, rows] = jnp.dot(
            value_flip_ref[...], rounded, preferred_element_type=wide
        ).astype(jnp.bfloat16)
        return carry

    lax.fori_loop(0, pixels // block, attend, 0)
    own = pl.ds(pl.multiple_of(height * own_pixels, own_pixels), own_pixels)
    output_ref[...] = (
        residual_ref[own, :]
        + lax.dot_general(
            out_flip_ref[:, own],
            proj_ref[...],
            (((0,), (0,)), ((), ())),
            preferred_element_type=wide,
        )
        + proj_bias_ref[...]
    ).astype(jnp.bfloat16)


def send_order(source_ref, targets, axis, share):
    me = lax.axis_index("canvas")
    for step, target in enumerate(targets):
        place = pl.ds(pl.multiple_of((me ^ step) * share, share), share)
        target[...] = source_ref[place, :] if axis == 0 else source_ref[:, place]


def attention_kernel(
    grad_hbm,
    proj_hbm,
    normed_ref,
    query_ref,
    key_ref,
    value_ref,
    soft_ref,
    out_flip_ref,
    packed_ref,
    sums_ref,
    *refs,
    score_scale,
):
    *mixed_refs, mixed_ref, grad_ref, proj_ref, key_flip_ref, key_sum_ref, value_sum_ref, flip_ref, sems = refs
    pixels, channels = normed_ref.shape
    block = min(QUERY_ROWS, pixels)
    wide = jnp.float32
    copies = [
        pltpu.make_async_copy(grad_hbm, grad_ref, sems.at[0]),
        pltpu.make_async_copy(proj_hbm, proj_ref, sems.at[1]),
    ]
    for copy in copies:
        copy.start()
    half = channels // 2
    core = lax.axis_index("height") & 1
    half_lanes = pl.ds(pl.multiple_of(core * half, half), half)
    flip_ref[...] = normed_ref[:, half_lanes].T
    key_flip_ref[...] = key_ref[...].T
    key_sum_ref[...] = jnp.zeros(key_sum_ref.shape, wide)
    value_sum_ref[...] = jnp.zeros(value_sum_ref.shape, wide)
    for copy in copies:
        copy.wait()

    def attend(index, carry):
        rows = pl.ds(pl.multiple_of(index * block, block), block)
        back = lax.dot_general(
            grad_ref[rows, :], proj_ref[...], (((1,), (1,)), ((), ())), preferred_element_type=wide
        ).astype(jnp.bfloat16)
        rounded = soft_ref[:, rows]
        weights = rounded.astype(wide)
        weight_grad = lax.dot_general(
            value_ref[...], back, (((1,), (1,)), ((), ())), preferred_element_type=wide
        )
        value_sum_ref[...] += jnp.dot(rounded, back, preferred_element_type=wide)
        dots = jnp.sum(weights * weight_grad, axis=0, keepdims=True)
        score_grad = (weights * (weight_grad - dots)).astype(jnp.bfloat16)
        key_sum_ref[...] += jnp.dot(score_grad, query_ref[rows, :], preferred_element_type=wide)
        query_grad = jnp.dot(key_flip_ref[...], score_grad, preferred_element_type=wide)
        packed_ref[rows, 0:channels] = (query_grad * score_scale).astype(jnp.bfloat16).T
        return carry

    lax.fori_loop(0, pixels // block, attend, 0)

    def pack(rows, carry):
        packed_ref[rows, channels : 2 * channels] = (key_sum_ref[rows, :] * score_scale).astype(
            jnp.bfloat16
        )
        packed_ref[rows, 2 * channels :] = value_sum_ref[rows, :].astype(jnp.bfloat16)
        return (
            carry[0] + fold(packed_ref[rows, 0:channels].astype(wide)),
            carry[1] + fold(packed_ref[rows, 2 * channels :].astype(wide)),
            carry[2] + fold(grad_ref[rows, :].astype(wide)),
        )

    zeros = jnp.zeros((8, channels), wide)
    totals = each_chunk(pixels, pack, (zeros, zeros, zeros))
    sums_ref[...] = jnp.zeros(sums_ref.shape, wide)
    for row, total in enumerate(totals):
        sums_ref[8 + row : 9 + row, :] = column_total(total)

    half_rows = pl.ds(pl.multiple_of(core * half, half), half)
    mixed_ref[:, 0 : 3 * channels] = jnp.dot(
        flip_ref[...], packed_ref[...], preferred_element_type=wide
    ).astype(jnp.bfloat16)
    mixed_ref[:, 3 * channels :] = jnp.dot(
        out_flip_ref[half_rows, :], grad_ref[...], preferred_element_type=wide
    ).astype(jnp.bfloat16)
    send_order(mixed_ref, mixed_refs, 0, half // len(mixed_refs))


def third_kernel(
    grad_hbm,
    qkv_hbm,
    packed_ref,
    residual_ref,
    table_ref,
    act_two_ref,
    mask_ref,
    old_sums_ref,
    residual_grad_ref,
    grad_two_ref,
    sums_ref,
    *refs,
    cols,
):
    *part_refs, grad_ref, qkv_ref, total_ref, narrow_ref, columns_ref, part_ref, sems = refs
    pixels, channels = residual_ref.shape
    block = min(CONV_ROWS, pixels)
    wide = jnp.float32
    copies = [
        pltpu.make_async_copy(qkv_hbm, qkv_ref, sems.at[0]),
        pltpu.make_async_copy(grad_hbm, grad_ref, sems.at[1]),
    ]
    for copy in copies:
        copy.start()
    mean, inverse, gain, shift = norm_rows(table_ref, 2)
    zeros = jnp.zeros((8, channels), wide)
    copies[0].wait()

    def input_grads(index, carry):
        rows = pl.ds(pl.multiple_of(index * block, block), block)
        normed_grad = lax.dot_general(
            packed_ref[rows, :], qkv_ref[...], (((1,), (1,)), ((), ())), preferred_element_type=wide
        )
        total_ref[rows, :] = normed_grad
        normed = (residual_ref[rows, :] - mean) * inverse
        return carry[0] + fold(normed_grad), carry[1] + fold(normed_grad * normed)

    sums = lax.fori_loop(0, pixels // block, input_grads, (zeros, zeros))
    sums_ref[...] = old_sums_ref[...]
    sums_ref[5:6, :] = column_total(sums[1])
    sums_ref[6:7, :] = column_total(sums[0])
    mean_grad, mean_cross = back_means(sums, gain, pixels)
    copies[1].wait()

    def finish(rows, carry):
        normed = (residual_ref[rows, :] - mean) * inverse
        back = inverse * (total_ref[rows, :] * gain - mean_grad - normed * mean_cross)
        total = grad_ref[rows, :].astype(wide) + back
        residual_grad_ref[rows, :] = total
        low = total.astype(jnp.bfloat16)
        grad_two_ref[rows, :] = low
        return carry + fold(low.astype(wide))

    sums_ref[7:8, :] = column_total(each_chunk(pixels, finish, zeros))
    weight_part(
        act_two_ref, grad_two_ref, mask_ref, narrow_ref, columns_ref, part_ref, part_refs, cols
    )


def second_kernel(
    grad_two_ref,
    middle_ref,
    table_ref,
    act_one_ref,
    mask_ref,
    old_sums_ref,
    weights_hbm,
    grad_one_ref,
    sums_ref,
    *refs,
    cols,
):
    *part_refs, weights_ref, taps_ref, total_ref, narrow_ref, columns_ref, part_ref, sem = refs
    pixels, channels = middle_ref.shape
    copy = pltpu.make_async_copy(weights_hbm.at[1], weights_ref, sem)
    copy.start()
    sums, back = conv_back(
        grad_two_ref,
        copy,
        weights_ref,
        mask_ref,
        taps_ref,
        total_ref,
        lambda rows: middle_ref[rows, :],
        table_ref,
        1,
        cols,
    )
    sums_ref[...] = old_sums_ref[...]
    sums_ref[2:3, :] = column_total(sums[1])
    sums_ref[3:4, :] = column_total(sums[0])

    def finish(rows, carry):
        low = back(rows).astype(jnp.bfloat16)
        grad_one_ref[rows, :] = low
        return carry + fold(low.astype(jnp.float32))

    zeros = jnp.zeros((8, channels), jnp.float32)
    sums_ref[4:5, :] = column_total(each_chunk(pixels, finish, zeros))
    weight_part(
        act_one_ref, grad_one_ref, mask_ref, narrow_ref, columns_ref, part_ref, part_refs, cols
    )


def first_kernel(
    grad_one_ref,
    features_ref,
    residual_grad_ref,
    table_ref,
    mask_ref,
    old_sums_ref,
    weights_hbm,
    input_grad_ref,
    sums_ref,
    weights_ref,
    taps_ref,
    total_ref,
    sem,
    *,
    cols,
):
    copy = pltpu.make_async_copy(weights_hbm.at[0], weights_ref, sem)
    copy.start()
    sums, back = conv_back(
        grad_one_ref,
        copy,
        weights_ref,
        mask_ref,
        taps_ref,
        total_ref,
        lambda rows: features_ref[rows, :].astype(jnp.float32),
        table_ref,
        0,
        cols,
    )
    sums_ref[...] = old_sums_ref[...]
    sums_ref[0:1, :] = column_total(sums[1])
    sums_ref[1:2, :] = column_total(sums[0])
    count = input_grad_ref.shape[0]
    own = pl.ds(pl.multiple_of(lax.axis_index("height") * count, count), count)
    input_grad_ref[...] = (residual_grad_ref[own, :] + back(own)).astype(jnp.bfloat16)


def place_kernel(*refs):
    pieces, (qkv_hbm, proj_hbm, packed_ref, qkv_ref, proj_ref, sems) = refs[:-6], refs[-6:]
    inner = qkv_ref.shape[1]
    share = pieces[0].shape[0]
    half = packed_ref.shape[0]
    me = lax.axis_index("canvas")
    for step, piece in enumerate(pieces):
        place = pl.ds(pl.multiple_of((me ^ step) * share, share), share)
        packed_ref[place, :] = piece[...]
    core = lax.axis_index("height") & 1
    spread_half(core, packed_ref, qkv_ref, proj_ref, qkv_hbm, proj_hbm, sems)


def spread_half(owner, packed_ref, qkv_ref, proj_ref, qkv_hbm, proj_hbm, sems):
    half = packed_ref.shape[0]
    inner = qkv_ref.shape[1]
    rows = pl.ds(pl.multiple_of(owner * half, half), half)
    qkv_ref[...] = packed_ref[:, 0:inner].astype(jnp.float32)
    copies = [pltpu.make_async_copy(qkv_ref, qkv_hbm.at[rows, :], sems.at[0])]
    copies[0].start()
    proj_ref[...] = packed_ref[:, inner:].astype(jnp.float32)
    copies.append(pltpu.make_async_copy(proj_ref, proj_hbm.at[rows, :], sems.at[1]))
    copies[1].start()
    for copy in copies:
        copy.wait()


def join_kernel(*refs):
    ins, (qkv_hbm, proj_hbm, conv_ref, qkv_ref, proj_ref, sems) = refs[:-6], refs[-6:]
    packed_ref, parts = ins[2], ins[3:]
    count = len(parts) // 2
    for which in range(2):
        total = parts[which * count][...].astype(jnp.float32)
        for part in parts[which * count + 1 : (which + 1) * count]:
            total = total + part[...].astype(jnp.float32)
        conv_ref[which] = total.reshape(conv_ref.shape[1:])
    core = lax.axis_index("height") & 1
    spread_half(1 - core, packed_ref, qkv_ref, proj_ref, qkv_hbm, proj_hbm, sems)


def sums_kernel(*refs):
    gains_ref, shifts_ref, conv_ref, qv_ref, proj_ref = refs[-5:]
    total = refs[0][...]
    for ref in refs[1:-5]:
        total = total + ref[...]
    for row, start in enumerate((0, 2, 5)):
        gains_ref[row : row + 1, :] = total[start : start + 1]
        shifts_ref[row : row + 1, :] = total[start + 1 : start + 2]
    conv_ref[0:1, :] = total[4:5]
    conv_ref[1:2, :] = total[7:8]
    qv_ref[...] = total[8:10]
    proj_ref[...] = total[10:11]


def call_kernel(kernel, outputs, scratch, operands, places, flops, limit, out_places=None, aliases={}):
    out_places = out_places or "v" * len(outputs)
    spaces = {
        "v": pl.BlockSpec(memory_space=pltpu.VMEM),
        "s": pl.BlockSpec(memory_space=pltpu.SMEM),
        "h": pl.BlockSpec(memory_space=pl.ANY),
        "o": pl.BlockSpec(memory_space=pltpu.VMEM),
        "a": pl.BlockSpec(memory_space=pl.ANY),
    }
    moved = sum(array.size * array.dtype.itemsize for array in operands)
    held = {"v": pltpu.VMEM, "h": pltpu.HBM, "o": jax.ShapeDtypeStruct}
    operands = [
        pltpu.with_memory_space_constraint(array, pltpu.HBM) if place == "h" else array
        for array, place in zip(operands, places)
    ]
    return pl.pallas_call(
        kernel,
        out_shape=[held[place](*output) for output, place in zip(outputs, out_places)],
        in_specs=[spaces[place] for place in places],
        out_specs=[spaces[place] for place in out_places],
        scratch_shapes=scratch,
        input_output_aliases=aliases,
        compiler_params=pltpu.CompilerParams(vmem_limit_bytes=limit * 2**20),
        cost_estimate=pl.CostEstimate(flops=flops, bytes_accessed=moved, transcendentals=0),
    )(*operands)


def gather_height(block, size):
    held = [block] + [
        lax.ppermute(block, "height", [(i, i ^ step) for i in range(size)])
        for step in range(2, size, 2)
    ]
    pieces = []
    for piece in held:
        pieces.append(piece)
        pieces.append(lax.ppermute(piece, "height", [(i, i ^ 1) for i in range(size)]))
    return pieces


def trade_canvas(pieces):
    size = lax.axis_size("canvas")
    return [pieces[0]] + [
        lax.ppermute(piece, "canvas", [(i, i ^ step) for i in range(size)])
        for step, piece in enumerate(pieces)
        if step
    ]


def whole_canvas(
    features,
    tile_ids,
    norm_gains,
    norm_shifts,
    conv_weights,
    conv_biases,
    qkv_weight,
    qv_bias,
    proj_weight,
    proj_bias,
    cotangent,
):
    height_size = lax.axis_size("height")
    canvas_size = lax.axis_size("canvas")
    local_rows, cols, channels = features.shape[1:]
    all_rows = tile_ids.shape[1]
    pixels = all_rows * cols
    own_pixels = local_rows * cols
    out_share = channels // height_size
    ci_share = channels // canvas_size
    row_share = channels // 2 // canvas_size
    low, wide = jnp.bfloat16, jnp.float32

    pieces = gather_height(features.reshape(own_pixels, channels), height_size)
    late_cotangent, *pieces = lax.optimization_barrier((cotangent[0], *pieces))
    out_grad = lax.all_gather(late_cotangent, "height", axis=0, tiled=True)
    out_grad = out_grad.reshape(pixels, channels)

    plane = ((pixels, channels), low)
    plane_wide = ((pixels, channels), wide)
    sums_shape = ((16, channels), wide)
    part_shapes = [((9 * out_share, ci_share), low)] * canvas_size
    mixed_shapes = [((row_share, 4 * channels), low)] * canvas_size
    taps = pltpu.VMEM((pixels + 2 * cols, 3 * channels), low)
    held = pltpu.VMEM((pixels, channels), low)
    held_wide = pltpu.VMEM((pixels, channels), wide)
    flipped = pltpu.VMEM((channels, pixels), low)
    half_flipped = pltpu.VMEM((channels // 2, pixels), low)
    half_mixed = pltpu.VMEM((channels // 2, 4 * channels), low)
    half_qkv = pltpu.VMEM((channels // 2, 3 * channels), wide)
    half_proj = pltpu.VMEM((channels // 2, channels), wide)
    conv_held = pltpu.VMEM(conv_weights.shape[1:], low)
    narrow = pltpu.VMEM((pixels + 2 * cols, 3 * NARROW), wide)
    columns = pltpu.VMEM((pixels, 5 * NARROW), low)
    part_held = pltpu.VMEM((5 * NARROW, channels), low)
    sem = pltpu.SemaphoreType.DMA
    conv_flops = 2 * 9 * pixels * channels * channels
    dot_flops = 2 * pixels * channels * channels
    score_flops = 2 * pixels * pixels * channels
    scale = channels ** (-0.5)

    (
        all_features,
        act_one,
        middle,
        act_two,
        residual,
        normed,
        table,
        mask,
        query,
        key,
        value,
        soft,
        out_flip,
        output,
    ) = call_kernel(
        functools.partial(forward_kernel, cols=cols, score_scale=scale, count=height_size),
        [
            plane,
            plane,
            plane_wide,
            plane,
            plane_wide,
            plane,
            ((16, channels), wide),
            ((2, pixels, LANES), wide),
            plane,
            plane,
            plane,
            ((pixels, pixels), low),
            ((channels, pixels), low),
            ((own_pixels, channels), low),
        ],
        [
            pltpu.SMEM(tile_ids.shape, jnp.int32),
            pltpu.VMEM(norm_gains.shape, wide),
            pltpu.VMEM(norm_shifts.shape, wide),
            pltpu.VMEM(conv_biases.shape, wide),
            pltpu.VMEM(qv_bias.shape, wide),
            pltpu.VMEM((1, channels), wide),
            pltpu.VMEM(conv_weights.shape, low),
            pltpu.VMEM(qkv_weight.shape, low),
            pltpu.VMEM(proj_weight.shape, low),
            taps,
            pltpu.VMEM((pixels, LANES), jnp.int32),
            pltpu.VMEM((8, pixels), jnp.int32),
            flipped,
            sem((10,)),
            sem((height_size,)),
        ],
        [
            *pieces,
            tile_ids,
            norm_gains,
            norm_shifts,
            conv_biases,
            qv_bias,
            proj_bias.reshape(1, channels),
            conv_weights,
            qkv_weight,
            proj_weight,
        ],
        "h" + "a" * (height_size - 1) + "h" * 9,
        2 * conv_flops + 3 * dot_flops + 2 * score_flops,
        24,
        "v" * 13 + "o",
    )
    packed, sums, *mixed = call_kernel(
        functools.partial(attention_kernel, score_scale=scale),
        [((pixels, 3 * channels), low), sums_shape, *mixed_shapes],
        [
            half_mixed,
            held,
            pltpu.VMEM(proj_weight.shape, low),
            flipped,
            held_wide,
            held_wide,
            half_flipped,
            sem((2,)),
        ],
        [out_grad, proj_weight, normed, query, key, value, soft, out_flip],
        "hhvvvvvv",
        3 * dot_flops + 4 * score_flops,
        20,
    )
    mixed = trade_canvas(mixed)
    residual_grad, grad_two, sums, *parts_two = call_kernel(
        functools.partial(third_kernel, cols=cols),
        [plane_wide, plane, sums_shape, *part_shapes],
        [
            held,
            pltpu.VMEM(qkv_weight.shape, low),
            held_wide,
            narrow,
            columns,
            part_held,
            sem((2,)),
        ],
        [out_grad, qkv_weight, packed, residual, table, act_two, mask, sums],
        "hhvvvvvv",
        3 * dot_flops + conv_flops // height_size,
        16,
    )
    parts_two = trade_canvas(parts_two)
    *mixed, grad_two = lax.optimization_barrier((*mixed, grad_two))
    mixed_sum = mixed[0].astype(wide)
    for piece in mixed[1:]:
        mixed_sum = mixed_sum + piece.astype(wide)
    mixed_sum = trade_canvas([mixed_sum.astype(low)] * canvas_size)
    back_scratch = [conv_held, taps, held_wide]
    grad_one, sums, *parts_one = call_kernel(
        functools.partial(second_kernel, cols=cols),
        [plane, sums_shape, *part_shapes],
        back_scratch + [narrow, columns, part_held, sem],
        [grad_two, middle, table, act_one, mask, sums, conv_weights],
        "vvvvvvh",
        conv_flops + conv_flops // height_size,
        24,
    )
    parts_one = trade_canvas(parts_one)
    *mixed_sum, grad_one = lax.optimization_barrier((*mixed_sum, grad_one))
    qkv_grad, proj_grad, mixed_half = call_kernel(
        place_kernel,
        [(qkv_weight.shape, wide), (proj_weight.shape, wide), ((channels // 2, 4 * channels), low)],
        [half_qkv, half_proj, sem((2,))],
        mixed_sum,
        "v" * canvas_size,
        0,
        12,
        "hhv",
    )
    mixed_other = lax.ppermute(mixed_half, "height", [(i, i ^ 1) for i in range(height_size)])
    input_grad, sums = call_kernel(
        functools.partial(first_kernel, cols=cols),
        [((own_pixels, channels), low), sums_shape],
        back_scratch + [sem],
        [grad_one, all_features, residual_grad, table, mask, sums, conv_weights],
        "vvvvvvh",
        conv_flops,
        20,
        "ov",
    )
    all_sums = trade_canvas([sums] * canvas_size)
    qkv_grad, proj_grad, conv_grad = call_kernel(
        join_kernel,
        [
            (qkv_weight.shape, wide),
            (proj_weight.shape, wide),
            ((2, 3, 3, out_share, ci_share), wide),
        ],
        [half_qkv, half_proj, sem((2,))],
        [qkv_grad, proj_grad, mixed_other, *parts_one, *parts_two],
        "hhv" + "v" * (2 * canvas_size),
        0,
        12,
        "hho",
        {0: 0, 1: 1},
    )
    vector_shapes = [norm_gains.shape, norm_shifts.shape, conv_biases.shape, qv_bias.shape]
    gains_grad, shifts_grad, biases_grad, qv_grad, proj_bias_grad = call_kernel(
        sums_kernel,
        [(shape, wide) for shape in vector_shapes + [(1, channels)]],
        [],
        all_sums,
        "v" * canvas_size,
        0,
        16,
        "ooooo",
    )
    own_shape = (1, local_rows, cols, channels)
    return (
        output.reshape(own_shape),
        input_grad.reshape(own_shape),
        gains_grad,
        shifts_grad,
        jnp.swapaxes(conv_grad, 3, 4),
        biases_grad,
        qkv_grad,
        qv_grad,
        proj_grad,
        proj_bias_grad.reshape(channels),
    )


def on_device(*arrays):
    features, tile_ids = arrays[0], arrays[1]
    local_rows, cols, channels = features.shape[1:]
    pixels = tile_ids.shape[1] * cols
    height_size, canvas_size = lax.axis_size("height"), lax.axis_size("canvas")
    powers = all(size & (size - 1) == 0 for size in (height_size, canvas_size, cols))
    fits = (
        powers
        and height_size > 1
        and pixels <= MOST_PIXELS
        and pixels % CONV_ROWS == 0
        and (local_rows * cols) % LANES == 0
        and CHUNK % cols == 0
        and cols % 16 == 0
        and channels % (LANES * canvas_size) == 0
        and 2 * channels == NARROW * height_size
    )
    return whole_canvas(*arrays) if fits else split_canvas(*arrays)


def solution(mesh):
    in_specs = (
        P("canvas", "height", None, None),
        P("canvas", None),
        P(),
        P(),
        P(),
        P(),
        P(),
        P(),
        P(),
        P(),
        P("canvas", "height", None, None),
    )
    out_specs = (
        P("canvas", "height", None, None),
        P("canvas", "height", None, None),
        P(),
        P(),
        P(None, None, None, "canvas", "height"),
        P(),
        P(),
        P(),
        P(),
        P(),
    )
    return jax.shard_map(
        on_device, mesh=mesh, in_specs=in_specs, out_specs=out_specs, check_vma=False
    )
```

```python
import functools

import jax
import jax.numpy as jnp
from jax import lax
from jax.experimental import pallas as pl
from jax.experimental.pallas import tpu as pltpu
from jax.sharding import PartitionSpec as P

GROUPS = 32


epsilon = 1e-06
masked_score = -1e30
MOST_PIXELS = 1024
LANES = 128
NARROW = 128
CHUNK = 128
CONV_ROWS = 512
QUERY_ROWS = 256


def extended(block, sides, width):
    for axis, dim in sides:
        count = lax.axis_size(axis)
        forward = [(i, i + 1) for i in range(count - 1)]
        backward = [(target, source) for source, target in forward]
        low = lax.ppermute(
            lax.slice_in_dim(block, block.shape[dim] - width, None, axis=dim), axis, forward
        )
        high = lax.ppermute(lax.slice_in_dim(block, 0, width, axis=dim), axis, backward)
        block = jnp.concatenate([low, block, high], axis=dim)
    return block


def group_total(vector):
    return vector.reshape(GROUPS, -1).sum(axis=1)


def spread_groups(vector, channels):
    return jnp.repeat(vector, channels // GROUPS)


def norm_forward(values, gain, shift, members):
    channels = values.shape[1]
    totals = lax.psum(group_total(jnp.sum(values, axis=0)), "height")
    centered = values - spread_groups(totals / members, channels)
    squares = lax.psum(group_total(jnp.sum(centered * centered, axis=0)), "height")
    inverse = spread_groups(lax.rsqrt(squares / members + epsilon), channels)
    normed = centered * inverse
    return (normed, inverse, normed * gain + shift)


def norm_backward(grad_in, normed, inverse, gain, members):
    channels = grad_in.shape[1]
    scaled = grad_in * gain
    both_sums = lax.psum(
        (group_total(jnp.sum(scaled, axis=0)), group_total(jnp.sum(scaled * normed, axis=0))),
        "height",
    )
    mean_grad = spread_groups(both_sums[0] / members, channels)
    mean_cross = spread_groups(both_sums[1] / members, channels)
    result = inverse * (scaled - mean_grad - normed * mean_cross)
    return (result, jnp.sum(grad_in * normed, axis=0), jnp.sum(grad_in, axis=0))


def swish(values):
    return values * jax.nn.sigmoid(values)


def swish_slope(values):
    sigmoid_part = jax.nn.sigmoid(values)
    return sigmoid_part * (1.0 + values * (1.0 - sigmoid_part))


def tap_columns(padded, row_mask, local_rows, canvas_cols):
    pieces = []
    for row_tap in range(3):
        rows_taken = padded[row_tap : row_tap + local_rows] * row_mask[:, row_tap, None, None]
        for col_tap in range(3):
            pieces.append(rows_taken[:, col_tap : col_tap + canvas_cols])
    stacked = jnp.concatenate(pieces, axis=2)
    return stacked.reshape(local_rows * canvas_cols, stacked.shape[2])


def conv_forward(acts, row_mask, weight, bias):
    local_rows, canvas_cols, channels = acts.shape
    rimmed = extended(acts, (("height", 0),), 1)
    padded = jnp.pad(rimmed, ((0, 0), (1, 1), (0, 0)))
    gathered = tap_columns(padded, row_mask, local_rows, canvas_cols)
    result = (
        jnp.dot(
            gathered, weight.reshape(9 * channels, channels), preferred_element_type=jnp.float32
        )
        + bias
    )
    return (result, gathered)


def conv_backward(grad_low, row_mask, weight, gathered):
    local_rows, canvas_cols, channels = grad_low.shape
    flat_grad = grad_low.reshape(local_rows * canvas_cols, channels)
    weight_grad = lax.dot_general(
        gathered, flat_grad, (((0,), (0,)), ((), ())), preferred_element_type=jnp.float32
    )
    rimmed = extended(grad_low, (("height", 0),), 1)
    padded = jnp.pad(rimmed, ((0, 0), (1, 1), (0, 0)))
    grad_taps = tap_columns(padded, row_mask, local_rows, canvas_cols)
    flipped = jnp.transpose(weight[::-1, ::-1], (0, 1, 3, 2)).reshape(9 * channels, channels)
    input_part = jnp.dot(grad_taps, flipped, preferred_element_type=jnp.float32)
    return (
        input_part,
        weight_grad.reshape(3, 3, channels, channels),
        jnp.sum(flat_grad.astype(jnp.float32), axis=0),
    )


def take_rows(array, offset, count):
    return lax.dynamic_slice_in_dim(array, offset, count)


def score_grads(
    queries, out_grad, log_total, row_dots, query_ids, key_rows, value_rows, key_ids, score_scale
):
    scores = (
        lax.dot_general(
            queries, key_rows, (((1,), (1,)), ((), ())), preferred_element_type=jnp.float32
        )
        * score_scale
    )
    same_tile = query_ids[:, None] == key_ids[None, :]
    softmax_block = jnp.exp(jnp.where(same_tile, scores - log_total[:, None], masked_score))
    weight_grad = lax.dot_general(
        out_grad, value_rows, (((1,), (1,)), ((), ())), preferred_element_type=jnp.float32
    )
    score_grad = (softmax_block * (weight_grad - row_dots[:, None])).astype(jnp.bfloat16)
    return (softmax_block.astype(jnp.bfloat16), score_grad)


def split_canvas(
    features,
    tile_ids,
    norm_gains,
    norm_shifts,
    conv_weights,
    conv_biases,
    qkv_weight,
    qv_bias,
    proj_weight,
    proj_bias,
    cotangent,
):
    height_size = lax.axis_size("height")
    local_rows = features.shape[1]
    canvas_cols = features.shape[2]
    channels = features.shape[3]
    pixels = local_rows * canvas_cols
    row_ids = tile_ids[0]
    all_rows = row_ids.shape[0]
    members = float(all_rows * canvas_cols * (channels // GROUPS))
    score_scale = channels ** (-0.5)
    first_row = lax.axis_index("height") * local_rows
    edge_ids = jnp.full((1,), -1, jnp.int32)
    padded_ids = jnp.concatenate([edge_ids, row_ids, edge_ids])
    near_ids = lax.dynamic_slice_in_dim(padded_ids, first_row, local_rows + 2)
    own_rows = near_ids[1 : local_rows + 1]
    row_mask = jnp.stack(
        [near_ids[row_tap : row_tap + local_rows] == own_rows for row_tap in range(3)], axis=1
    ).astype(jnp.bfloat16)
    key_ids = jnp.repeat(row_ids, canvas_cols)
    query_ids = jnp.repeat(own_rows, canvas_cols)
    grid_shape = (local_rows, canvas_cols, channels)
    inputs = features[0].reshape(pixels, channels).astype(jnp.float32)
    normed_one, inverse_one, pre_one = norm_forward(inputs, norm_gains[0], norm_shifts[0], members)
    act_one = swish(pre_one).astype(jnp.bfloat16).reshape(grid_shape)
    middle, taps_one = conv_forward(act_one, row_mask, conv_weights[0], conv_biases[0])
    normed_two, inverse_two, pre_two = norm_forward(middle, norm_gains[1], norm_shifts[1], members)
    act_two = swish(pre_two).astype(jnp.bfloat16).reshape(grid_shape)
    branch, taps_two = conv_forward(act_two, row_mask, conv_weights[1], conv_biases[1])
    residual = inputs + branch
    normed_three, inverse_three, pre_three = norm_forward(
        residual, norm_gains[2], norm_shifts[2], members
    )
    attn_input = pre_three.astype(jnp.bfloat16)
    mixed = jnp.dot(attn_input, qkv_weight, preferred_element_type=jnp.float32)
    queries = (mixed[:, :channels] + qv_bias[0]).astype(jnp.bfloat16)
    key_rows = mixed[:, channels : 2 * channels].astype(jnp.bfloat16)
    value_rows = (mixed[:, 2 * channels :] + qv_bias[1]).astype(jnp.bfloat16)
    running_max = jnp.full((pixels,), masked_score, jnp.float32)
    key_piece = lax.all_gather(key_rows, "height", axis=0, tiled=True)
    value_piece = lax.all_gather(value_rows, "height", axis=0, tiled=True)
    scores = (
        lax.dot_general(
            queries, key_piece, (((1,), (1,)), ((), ())), preferred_element_type=jnp.float32
        )
        * score_scale
    )
    same_tile = query_ids[:, None] == key_ids[None, :]
    scores = jnp.where(same_tile, scores, masked_score)
    new_max = jnp.maximum(running_max, jnp.max(scores, axis=1))
    weights = jnp.where(same_tile, jnp.exp(scores - new_max[:, None]), 0.0)
    summed_out = jnp.dot(
        weights.astype(jnp.bfloat16), value_piece, preferred_element_type=jnp.float32
    )
    total_weight = jnp.sum(weights, axis=1)
    log_total = new_max + jnp.log(total_weight)
    attended = summed_out / total_weight[:, None]
    attended_low = attended.astype(jnp.bfloat16)
    output = (
        residual
        + jnp.dot(attended_low, proj_weight, preferred_element_type=jnp.float32)
        + proj_bias
    )
    out_grad = cotangent[0].reshape(pixels, channels)
    out_grad_full = out_grad.astype(jnp.float32)
    proj_grad = lax.dot_general(
        attended_low, out_grad, (((0,), (0,)), ((), ())), preferred_element_type=jnp.float32
    )
    proj_bias_grad = jnp.sum(out_grad_full, axis=0)
    attended_grad = lax.dot_general(
        out_grad, proj_weight, (((1,), (1,)), ((), ())), preferred_element_type=jnp.float32
    ).astype(jnp.bfloat16)
    row_dots = jnp.sum(attended_grad.astype(jnp.float32) * attended, axis=1)
    block_rows = pixels * min(height_size, 8)
    zero_block = jnp.zeros((pixels, channels), jnp.float32)
    key_all, value_all = (
        lax.all_gather(key_rows, "height", axis=0, tiled=True),
        lax.all_gather(value_rows, "height", axis=0, tiled=True),
    )
    query_all, grad_all = (
        lax.all_gather(queries, "height", axis=0, tiled=True),
        lax.all_gather(attended_grad, "height", axis=0, tiled=True),
    )
    total_all, dots_all = (
        lax.all_gather(log_total, "height", axis=0, tiled=True),
        lax.all_gather(row_dots, "height", axis=0, tiled=True),
    )

    def own_query_step(running, block_index):
        offset = block_index * block_rows
        key_part = take_rows(key_all, offset, block_rows)
        rounded, score_grad = score_grads(
            queries,
            attended_grad,
            log_total,
            row_dots,
            query_ids,
            key_part,
            take_rows(value_all, offset, block_rows),
            take_rows(key_ids, offset, block_rows),
            score_scale,
        )
        return (
            running
            + jnp.dot(score_grad, key_part, preferred_element_type=jnp.float32) * score_scale,
            None,
        )

    def own_key_step(running, block_index):
        offset = block_index * block_rows
        query_part = take_rows(query_all, offset, block_rows)
        grad_part = take_rows(grad_all, offset, block_rows)
        rounded, score_grad = score_grads(
            query_part,
            grad_part,
            take_rows(total_all, offset, block_rows),
            take_rows(dots_all, offset, block_rows),
            take_rows(key_ids, offset, block_rows),
            key_rows,
            value_rows,
            query_ids,
            score_scale,
        )
        key_part = (
            lax.dot_general(
                score_grad, query_part, (((0,), (0,)), ((), ())), preferred_element_type=jnp.float32
            )
            * score_scale
        )
        value_part = lax.dot_general(
            rounded, grad_part, (((0,), (0,)), ((), ())), preferred_element_type=jnp.float32
        )
        return ((running[0] + key_part, running[1] + value_part), None)

    block_count = key_all.shape[0] // block_rows
    query_grad, unused_one = lax.scan(own_query_step, zero_block, jnp.arange(block_count))
    (key_grad, value_grad), unused_two = lax.scan(
        own_key_step, (zero_block, zero_block), jnp.arange(block_count)
    )
    query_low = query_grad.astype(jnp.bfloat16)
    key_low = key_grad.astype(jnp.bfloat16)
    value_low = value_grad.astype(jnp.bfloat16)
    stacked_grad = jnp.concatenate([query_low, key_low, value_low], axis=1)
    qkv_grad = lax.dot_general(
        attn_input, stacked_grad, (((0,), (0,)), ((), ())), preferred_element_type=jnp.float32
    )
    qv_grad = jnp.stack(
        [
            jnp.sum(query_low.astype(jnp.float32), axis=0),
            jnp.sum(value_low.astype(jnp.float32), axis=0),
        ]
    )
    normed_grad = lax.dot_general(
        stacked_grad, qkv_weight, (((1,), (1,)), ((), ())), preferred_element_type=jnp.float32
    )
    back_three, gain_three, shift_three = norm_backward(
        normed_grad, normed_three, inverse_three, norm_gains[2], members
    )
    residual_grad = out_grad_full + back_three
    grad_two = residual_grad.astype(jnp.bfloat16).reshape(grid_shape)
    act_two_grad, weight_two_grad, bias_two_grad = conv_backward(
        grad_two, row_mask, conv_weights[1], taps_two
    )
    middle_grad, gain_two, shift_two = norm_backward(
        act_two_grad * swish_slope(pre_two), normed_two, inverse_two, norm_gains[1], members
    )
    grad_one = middle_grad.astype(jnp.bfloat16).reshape(grid_shape)
    act_one_grad, weight_one_grad, bias_one_grad = conv_backward(
        grad_one, row_mask, conv_weights[0], taps_one
    )
    input_back, gain_one, shift_one = norm_backward(
        act_one_grad * swish_slope(pre_one), normed_one, inverse_one, norm_gains[0], members
    )
    input_grad = residual_grad + input_back
    conv_grad = jnp.stack([weight_one_grad, weight_two_grad])
    conv_part = lax.psum_scatter(conv_grad, "height", scatter_dimension=4, tiled=True)
    conv_part = lax.psum_scatter(
        conv_part.astype(jnp.bfloat16), "canvas", scatter_dimension=3, tiled=True
    ).astype(jnp.float32)
    summed = lax.psum(
        (
            jnp.stack([gain_one, gain_two, gain_three]),
            jnp.stack([shift_one, shift_two, shift_three]),
            jnp.stack([bias_one_grad, bias_two_grad]),
            qkv_grad,
            qv_grad,
            proj_grad,
            proj_bias_grad,
        ),
        ("canvas", "height"),
    )
    return (
        output.astype(jnp.bfloat16).reshape((1,) + grid_shape),
        input_grad.astype(jnp.bfloat16).reshape((1,) + grid_shape),
        summed[0],
        summed[1],
        conv_part,
        summed[2],
        summed[3],
        summed[4],
        summed[5],
        summed[6],
    )


def fold(block):
    rows, width = block.shape
    return jnp.sum(block.reshape(rows // 8, 8, width), axis=0)


def group_lanes(block, group):
    lane = lax.broadcasted_iota(jnp.int32, block.shape, 1)
    width = block.shape[1]
    step = 1
    while step < group:
        above = pltpu.roll(block, step, 1)
        below = pltpu.roll(block, width - step, 1)
        block = block + jnp.where((lane & step) != 0, above, below)
        step *= 2
    return block


def group_mean(partial, members):
    spread = group_lanes(partial, partial.shape[1] // GROUPS)
    return jnp.sum(spread, axis=0, keepdims=True) * (1.0 / members)


def widen(block, width):
    return jnp.concatenate([block] * (width // block.shape[1]), axis=1)


def each_chunk(pixels, body, carry):
    def step(index, carry):
        return body(pl.ds(pl.multiple_of(index * CHUNK, CHUNK), CHUNK), carry)

    return lax.fori_loop(0, pixels // CHUNK, step, carry)


def norm_stats(read, pixels, channels):
    members = float(pixels * (channels // GROUPS))
    zeros = jnp.zeros((8, channels), jnp.float32)
    total = each_chunk(pixels, lambda rows, carry: carry + fold(read(rows)), zeros)
    mean = group_mean(total, members)

    def squares(rows, carry):
        centered = read(rows) - mean
        return carry + fold(centered * centered)

    spread = group_mean(each_chunk(pixels, squares, zeros), members)
    return mean, lax.rsqrt(spread + epsilon)


def put_taps(taps_ref, block, rows, cols):
    count, channels = block.shape
    place = lax.broadcasted_iota(jnp.int32, block.shape, 0) & (cols - 1)
    left = jnp.where(place == 0, 0.0, pltpu.roll(block, 1, 0))
    right = jnp.where(place == cols - 1, 0.0, pltpu.roll(block, count - 1, 0))
    inner = pl.ds(pl.multiple_of(rows.start + cols, cols), count)
    taps_ref[inner, 0:channels] = left.astype(jnp.bfloat16)
    taps_ref[inner, channels : 2 * channels] = block.astype(jnp.bfloat16)
    taps_ref[inner, 2 * channels :] = right.astype(jnp.bfloat16)


def clear_edges(taps_ref, cols):
    edge = jnp.zeros((cols, taps_ref.shape[1]), taps_ref.dtype)
    taps_ref[0:cols, :] = edge
    taps_ref[taps_ref.shape[0] - cols :, :] = edge


def run_conv(taps_ref, product, mask_ref, total_ref, first, cols):
    pixels, channels = total_ref.shape
    block = min(CONV_ROWS, pixels)
    for row_tap in (1, 0, 2):

        def step(index, carry):
            start = pl.multiple_of(index * block, block)
            rows = pl.ds(start, block)
            shifted = pl.ds(pl.multiple_of(start + row_tap * cols, cols), block)
            part = product(taps_ref, shifted, row_tap)
            if row_tap == 1:
                total_ref[rows, :] = first(rows) + part
            else:
                total_ref[rows, :] += widen(mask_ref[row_tap // 2, rows, :], channels) * part
            return carry

        lax.fori_loop(0, pixels // block, step, 0)


def product_forward(weight_ref):
    channels = weight_ref.shape[-1]

    def product(taps_ref, shifted, row_tap):
        return jnp.dot(
            taps_ref[shifted, :],
            weight_ref[row_tap].reshape(3 * channels, channels),
            preferred_element_type=jnp.float32,
        )

    return product


def product_backward(weight_ref):
    channels = weight_ref.shape[-1]

    def product(taps_ref, shifted, row_tap):
        total = None
        for col_tap in range(3):
            part = lax.dot_general(
                taps_ref[shifted, col_tap * channels : (col_tap + 1) * channels],
                weight_ref[2 - row_tap, 2 - col_tap],
                (((1,), (1,)), ((), ())),
                preferred_element_type=jnp.float32,
            )
            total = part if total is None else total + part
        return total

    return product


def smooth(values):
    part = 0.5 * jnp.tanh(0.5 * values) + 0.5
    return values * part, part


def activate(read, mean, inverse, gain, shift, act_ref, taps_ref, cols):
    scale = inverse * gain

    def step(rows, carry):
        act = smooth((read(rows) - mean) * scale + shift)[0]
        act_ref[rows, :] = act.astype(jnp.bfloat16)
        put_taps(taps_ref, act, rows, cols)
        return carry

    each_chunk(act_ref.shape[0], step, 0)


def back_sums(read_pair, pixels, channels):
    zeros = jnp.zeros((8, channels), jnp.float32)

    def step(rows, carry):
        grad, normed = read_pair(rows)
        return carry[0] + fold(grad), carry[1] + fold(grad * normed)

    plain, cross = each_chunk(pixels, step, (zeros, zeros))
    return plain, cross


def back_means(sums, gain, pixels):
    channels = gain.shape[1]
    members = float(pixels * (channels // GROUPS))
    return group_mean(sums[0] * gain, members), group_mean(sums[1] * gain, members)


def column_total(partial):
    return jnp.sum(partial, axis=0, keepdims=True)


def weight_part(act_ref, grad_ref, mask_ref, narrow_ref, columns_ref, part_ref, out_refs, cols):
    pixels, channels = act_ref.shape
    height = lax.axis_index("height")
    share = NARROW // 2
    block = pl.ds(pl.multiple_of((height // 2) * NARROW, NARROW), NARROW)
    parity = height % 2
    edge = jnp.zeros((cols, 3 * NARROW), jnp.float32)
    narrow_ref[0:cols, :] = edge
    narrow_ref[cols + pixels :, :] = edge

    def spread(rows, carry):
        own = grad_ref[rows, block].astype(jnp.float32)
        half = lax.broadcasted_iota(jnp.int32, own.shape, 1) // share
        turned = pltpu.roll(own, share, 1)
        both = jnp.where(half == parity, own, turned)
        place = lax.broadcasted_iota(jnp.int32, own.shape, 0) & (cols - 1)
        left = jnp.where(place == 0, 0.0, pltpu.roll(both, 1, 0))
        right = jnp.where(place == cols - 1, 0.0, pltpu.roll(both, CHUNK - 1, 0))
        inner = pl.ds(pl.multiple_of(rows.start + cols, cols), CHUNK)
        narrow_ref[inner, 0:NARROW] = left
        narrow_ref[inner, NARROW : 2 * NARROW] = both
        narrow_ref[inner, 2 * NARROW :] = right
        return carry

    each_chunk(pixels, spread, 0)

    def gather(rows, carry):
        taps = []
        for row_tap in range(3):
            for col_tap in range(3):
                row_back, col_back = 2 - row_tap, 2 - col_tap
                shifted = pl.ds(pl.multiple_of(rows.start + row_back * cols, cols), CHUNK)
                block = narrow_ref[shifted, col_back * NARROW : (col_back + 1) * NARROW]
                if row_back != 1:
                    block = block * mask_ref[row_back // 2, rows, :]
                taps.append(block)
        lower = lax.broadcasted_iota(jnp.int32, taps[0].shape, 1) < share
        for pair in range(5):
            second = taps[min(2 * pair + 1, 8)]
            columns_ref[rows, pair * NARROW : (pair + 1) * NARROW] = jnp.where(
                lower, taps[2 * pair], second
            ).astype(jnp.bfloat16)
        return carry

    each_chunk(pixels, gather, 0)
    part_ref[...] = lax.dot_general(
        columns_ref[...],
        act_ref[...],
        (((0,), (0,)), ((), ())),
        preferred_element_type=jnp.float32,
    ).astype(jnp.bfloat16)
    rows, width = out_refs[0].shape
    send_order(part_ref.at[0:rows, :], out_refs, 1, width)


def conv_back(grad_ref, copy, weights_ref, mask_ref, taps_ref, total_ref, read, table_ref, which, cols):
    pixels, channels = total_ref.shape
    wide = jnp.float32
    clear_edges(taps_ref, cols)

    def spread(rows, carry):
        put_taps(taps_ref, grad_ref[rows, :].astype(wide), rows, cols)
        return carry

    each_chunk(pixels, spread, 0)
    copy.wait()
    run_conv(
        taps_ref, product_backward(weights_ref), mask_ref, total_ref, lambda rows: 0.0, cols
    )
    mean, inverse, gain, shift = norm_rows(table_ref, which)

    def slope(rows):
        normed = (read(rows) - mean) * inverse
        pre = normed * gain + shift
        part = smooth(pre)[1]
        grad = total_ref[rows, :] * (part * (1.0 + pre * (1.0 - part)))
        total_ref[rows, :] = grad
        return grad, normed

    sums = back_sums(slope, pixels, channels)
    mean_grad, mean_cross = back_means(sums, gain, pixels)

    def back(rows):
        normed = (read(rows) - mean) * inverse
        return inverse * (total_ref[rows, :] * gain - mean_grad - normed * mean_cross)

    return sums, back


def norm_rows(table_ref, which):
    picks = (2 * which, 2 * which + 1, 6 + which, 9 + which)
    return tuple(table_ref[pick : pick + 1, :] for pick in picks)


def build_masks(ids_ref, mask_ref, id_rows_ref, id_cols_ref, cols):
    rows = ids_ref.shape[1]
    for row in range(rows):
        here = ids_ref[0, row]
        place = slice(row * cols, (row + 1) * cols)
        id_rows_ref[place, :] = jnp.full((cols, LANES), here, jnp.int32)
        for side, other in ((0, row - 1), (1, row + 1)):
            same = jnp.float32(0.0)
            if 0 <= other < rows:
                same = jnp.where(ids_ref[0, other] == here, 1.0, 0.0).astype(jnp.float32)
            mask_ref[side, place, :] = jnp.full((cols, LANES), same, jnp.float32)
    lane = lax.broadcasted_iota(jnp.int32, (8, LANES), 1)
    each = LANES // cols
    for block in range(rows // each):
        ids = jnp.full((8, LANES), ids_ref[0, block * each], jnp.int32)
        for step in range(1, each):
            ids = jnp.where(lane >= step * cols, ids_ref[0, block * each + step], ids)
        id_cols_ref[:, block * LANES : (block + 1) * LANES] = ids


def place_pieces(pieces, whole_ref, sems):
    own_pixels = whole_ref.shape[0] // len(pieces)
    height = lax.axis_index("height")
    copies = []
    for place, piece in enumerate(pieces):
        start = pl.multiple_of((height ^ place) * own_pixels, own_pixels)
        rows = pl.ds(start, own_pixels)
        copies.append(pltpu.make_async_copy(piece, whole_ref.at[rows, :], sems.at[place]))
    return copies


def conv_kernel(*refs, cols, count):
    pieces, refs = refs[:count], refs[count:]
    (
        ids_hbm,
        gains_hbm,
        shifts_hbm,
        biases_hbm,
        weights_hbm,
        features_ref,
        act_one_ref,
        middle_ref,
        act_two_ref,
        residual_ref,
        table_ref,
        mask_ref,
        id_rows_ref,
        id_cols_ref,
        ids_ref,
        gains_ref,
        shifts_ref,
        biases_ref,
        weights_ref,
        taps_ref,
        sems,
        piece_sems,
    ) = refs
    pixels, channels = features_ref.shape
    wide = jnp.float32
    arrivals = place_pieces(pieces, features_ref, piece_sems)
    moves = [
        (ids_hbm, ids_ref),
        (gains_hbm, gains_ref),
        (shifts_hbm, shifts_ref),
        (weights_hbm.at[0], weights_ref.at[0]),
        (biases_hbm, biases_ref),
        (weights_hbm.at[1], weights_ref.at[1]),
    ]
    copies = [
        pltpu.make_async_copy(source, target, sems.at[index])
        for index, (source, target) in enumerate(moves)
    ]
    for copy in copies[:1] + arrivals + copies[1:]:
        copy.start()
    clear_edges(taps_ref, cols)
    copies[0].wait()
    build_masks(ids_ref, mask_ref, id_rows_ref, id_cols_ref, cols)
    for copy in arrivals:
        copy.wait()

    def read_input(rows):
        return features_ref[rows, :].astype(wide)

    def read_middle(rows):
        return middle_ref[rows, :]

    def read_residual(rows):
        return residual_ref[rows, :]

    table_ref[0:1, :], table_ref[1:2, :] = norm_stats(read_input, pixels, channels)
    copies[1].wait()
    copies[2].wait()
    table_ref[6:9, :] = gains_ref[...]
    table_ref[9:12, :] = shifts_ref[...]
    activate(read_input, *norm_rows(table_ref, 0), act_one_ref, taps_ref, cols)
    copies[3].wait()
    copies[4].wait()
    run_conv(
        taps_ref,
        product_forward(weights_ref.at[0]),
        mask_ref,
        middle_ref,
        lambda rows: biases_ref[0:1, :],
        cols,
    )
    table_ref[2:3, :], table_ref[3:4, :] = norm_stats(read_middle, pixels, channels)
    activate(read_middle, *norm_rows(table_ref, 1), act_two_ref, taps_ref, cols)
    copies[5].wait()
    run_conv(
        taps_ref,
        product_forward(weights_ref.at[1]),
        mask_ref,
        residual_ref,
        lambda rows: read_input(rows) + biases_ref[1:2, :],
        cols,
    )
    table_ref[4:5, :], table_ref[5:6, :] = norm_stats(read_residual, pixels, channels)


def score_kernel(
    qkv_hbm,
    qv_bias_hbm,
    proj_hbm,
    proj_bias_hbm,
    residual_ref,
    table_ref,
    id_rows_ref,
    id_cols_ref,
    normed_ref,
    query_ref,
    key_ref,
    value_ref,
    soft_ref,
    out_flip_ref,
    output_ref,
    qkv_ref,
    qv_bias_ref,
    proj_ref,
    proj_bias_ref,
    value_flip_ref,
    sems,
    *,
    score_scale,
):
    pixels, channels = residual_ref.shape
    own_pixels = output_ref.shape[0]
    wide = jnp.float32
    moves = [
        (qkv_hbm, qkv_ref),
        (qv_bias_hbm, qv_bias_ref),
        (proj_hbm, proj_ref),
        (proj_bias_hbm, proj_bias_ref),
    ]
    copies = [
        pltpu.make_async_copy(source, target, sems.at[index])
        for index, (source, target) in enumerate(moves)
    ]
    for copy in copies:
        copy.start()
    mean, inverse, gain, shift = norm_rows(table_ref, 2)
    scale = inverse * gain
    for copy in copies:
        copy.wait()
    block = min(QUERY_ROWS, pixels)

    def project(index, carry):
        rows = pl.ds(pl.multiple_of(index * block, block), block)
        normed = ((residual_ref[rows, :] - mean) * scale + shift).astype(jnp.bfloat16)
        normed_ref[rows, :] = normed
        query_ref[rows, :] = (
            jnp.dot(normed, qkv_ref[:, 0:channels], preferred_element_type=wide)
            + qv_bias_ref[0:1, :]
        ).astype(jnp.bfloat16)
        key_ref[rows, :] = jnp.dot(
            normed, qkv_ref[:, channels : 2 * channels], preferred_element_type=wide
        ).astype(jnp.bfloat16)
        values = (
            jnp.dot(normed, qkv_ref[:, 2 * channels :], preferred_element_type=wide)
            + qv_bias_ref[1:2, :]
        ).astype(jnp.bfloat16)
        value_ref[rows, :] = values
        value_flip_ref[:, rows] = values.T
        return carry

    lax.fori_loop(0, pixels // block, project, 0)

    def attend(index, carry):
        rows = pl.ds(pl.multiple_of(index * block, block), block)
        scores = lax.dot_general(
            key_ref[...], query_ref[rows, :], (((1,), (1,)), ((), ())), preferred_element_type=wide
        )
        same = widen(id_rows_ref[...], block) == id_cols_ref[0:1, rows]
        scores = jnp.where(same, scores * score_scale, masked_score)
        scores = jnp.exp(scores - jnp.max(scores, axis=0, keepdims=True))
        weights = scores * (1.0 / jnp.sum(scores, axis=0, keepdims=True))
        rounded = weights.astype(jnp.bfloat16)
        soft_ref[:, rows] = rounded
        out_flip_ref[:, rows] = jnp.dot(
            value_flip_ref[...], rounded, preferred_element_type=wide
        ).astype(jnp.bfloat16)
        return carry

    lax.fori_loop(0, pixels // block, attend, 0)
    height = lax.axis_index("height")
    own = pl.ds(pl.multiple_of(height * own_pixels, own_pixels), own_pixels)
    output_ref[...] = (
        residual_ref[own, :]
        + lax.dot_general(
            out_flip_ref[:, own],
            proj_ref[...],
            (((0,), (0,)), ((), ())),
            preferred_element_type=wide,
        )
        + proj_bias_ref[...]
    ).astype(jnp.bfloat16)


def send_order(source_ref, targets, axis, share):
    me = lax.axis_index("canvas")
    for step, target in enumerate(targets):
        place = pl.ds(pl.multiple_of((me ^ step) * share, share), share)
        target[...] = source_ref[place, :] if axis == 0 else source_ref[:, place]


def attention_kernel(
    proj_hbm,
    normed_ref,
    query_ref,
    key_ref,
    value_ref,
    soft_ref,
    out_flip_ref,
    *refs,
    score_scale,
    count,
):
    pieces, (grad_ref, packed_ref, sums_ref), refs = (
        refs[:count],
        refs[count : count + 3],
        refs[count + 3 :],
    )
    *mixed_refs, mixed_ref, proj_ref, key_flip_ref, key_sum_ref, value_sum_ref, flip_ref, sems = refs
    pixels, channels = normed_ref.shape
    block = min(QUERY_ROWS, pixels)
    wide = jnp.float32
    copies = place_pieces(pieces, grad_ref, sems)
    copies.append(pltpu.make_async_copy(proj_hbm, proj_ref, sems.at[count]))
    for copy in copies:
        copy.start()
    half = channels // 2
    core = lax.axis_index("height") & 1
    half_lanes = pl.ds(pl.multiple_of(core * half, half), half)
    flip_ref[...] = normed_ref[:, half_lanes].T
    key_flip_ref[...] = key_ref[...].T
    key_sum_ref[...] = jnp.zeros(key_sum_ref.shape, wide)
    value_sum_ref[...] = jnp.zeros(value_sum_ref.shape, wide)
    for copy in copies:
        copy.wait()

    def attend(index, carry):
        rows = pl.ds(pl.multiple_of(index * block, block), block)
        back = lax.dot_general(
            grad_ref[rows, :], proj_ref[...], (((1,), (1,)), ((), ())), preferred_element_type=wide
        ).astype(jnp.bfloat16)
        rounded = soft_ref[:, rows]
        weights = rounded.astype(wide)
        weight_grad = lax.dot_general(
            value_ref[...], back, (((1,), (1,)), ((), ())), preferred_element_type=wide
        )
        value_sum_ref[...] += jnp.dot(rounded, back, preferred_element_type=wide)
        dots = jnp.sum(weights * weight_grad, axis=0, keepdims=True)
        score_grad = (weights * (weight_grad - dots)).astype(jnp.bfloat16)
        key_sum_ref[...] += jnp.dot(score_grad, query_ref[rows, :], preferred_element_type=wide)
        query_grad = jnp.dot(key_flip_ref[...], score_grad, preferred_element_type=wide)
        packed_ref[rows, 0:channels] = (query_grad * score_scale).astype(jnp.bfloat16).T
        return carry

    lax.fori_loop(0, pixels // block, attend, 0)

    def pack(rows, carry):
        packed_ref[rows, channels : 2 * channels] = (key_sum_ref[rows, :] * score_scale).astype(
            jnp.bfloat16
        )
        packed_ref[rows, 2 * channels :] = value_sum_ref[rows, :].astype(jnp.bfloat16)
        return (
            carry[0] + fold(packed_ref[rows, 0:channels].astype(wide)),
            carry[1] + fold(packed_ref[rows, 2 * channels :].astype(wide)),
            carry[2] + fold(grad_ref[rows, :].astype(wide)),
        )

    zeros = jnp.zeros((8, channels), wide)
    totals = each_chunk(pixels, pack, (zeros, zeros, zeros))
    sums_ref[...] = jnp.zeros(sums_ref.shape, wide)
    for row, total in enumerate(totals):
        sums_ref[8 + row : 9 + row, :] = column_total(total)

    half_rows = pl.ds(pl.multiple_of(core * half, half), half)
    mixed_ref[:, 0 : 3 * channels] = jnp.dot(
        flip_ref[...], packed_ref[...], preferred_element_type=wide
    ).astype(jnp.bfloat16)
    mixed_ref[:, 3 * channels :] = jnp.dot(
        out_flip_ref[half_rows, :], grad_ref[...], preferred_element_type=wide
    ).astype(jnp.bfloat16)
    send_order(mixed_ref, mixed_refs, 0, half // len(mixed_refs))


def third_kernel(
    qkv_hbm,
    grad_ref,
    packed_ref,
    residual_ref,
    table_ref,
    act_two_ref,
    mask_ref,
    old_sums_ref,
    residual_grad_ref,
    grad_two_ref,
    sums_ref,
    *refs,
    cols,
):
    *part_refs, qkv_ref, total_ref, narrow_ref, columns_ref, part_ref, sem = refs
    pixels, channels = residual_ref.shape
    block = min(CONV_ROWS, pixels)
    wide = jnp.float32
    copy = pltpu.make_async_copy(qkv_hbm, qkv_ref, sem)
    copy.start()
    mean, inverse, gain, shift = norm_rows(table_ref, 2)
    zeros = jnp.zeros((8, channels), wide)
    copy.wait()

    def input_grads(index, carry):
        rows = pl.ds(pl.multiple_of(index * block, block), block)
        normed_grad = lax.dot_general(
            packed_ref[rows, :], qkv_ref[...], (((1,), (1,)), ((), ())), preferred_element_type=wide
        )
        total_ref[rows, :] = normed_grad
        normed = (residual_ref[rows, :] - mean) * inverse
        return carry[0] + fold(normed_grad), carry[1] + fold(normed_grad * normed)

    sums = lax.fori_loop(0, pixels // block, input_grads, (zeros, zeros))
    sums_ref[...] = old_sums_ref[...]
    sums_ref[5:6, :] = column_total(sums[1])
    sums_ref[6:7, :] = column_total(sums[0])
    mean_grad, mean_cross = back_means(sums, gain, pixels)

    def finish(rows, carry):
        normed = (residual_ref[rows, :] - mean) * inverse
        back = inverse * (total_ref[rows, :] * gain - mean_grad - normed * mean_cross)
        total = grad_ref[rows, :].astype(wide) + back
        residual_grad_ref[rows, :] = total
        low = total.astype(jnp.bfloat16)
        grad_two_ref[rows, :] = low
        return carry + fold(low.astype(wide))

    sums_ref[7:8, :] = column_total(each_chunk(pixels, finish, zeros))
    weight_part(
        act_two_ref, grad_two_ref, mask_ref, narrow_ref, columns_ref, part_ref, part_refs, cols
    )


def second_kernel(
    grad_two_ref,
    middle_ref,
    table_ref,
    act_one_ref,
    mask_ref,
    old_sums_ref,
    weights_hbm,
    grad_one_ref,
    sums_ref,
    *refs,
    cols,
):
    *part_refs, weights_ref, taps_ref, total_ref, narrow_ref, columns_ref, part_ref, sem = refs
    pixels, channels = middle_ref.shape
    copy = pltpu.make_async_copy(weights_hbm.at[1], weights_ref, sem)
    copy.start()
    sums, back = conv_back(
        grad_two_ref,
        copy,
        weights_ref,
        mask_ref,
        taps_ref,
        total_ref,
        lambda rows: middle_ref[rows, :],
        table_ref,
        1,
        cols,
    )
    sums_ref[...] = old_sums_ref[...]
    sums_ref[2:3, :] = column_total(sums[1])
    sums_ref[3:4, :] = column_total(sums[0])

    def finish(rows, carry):
        low = back(rows).astype(jnp.bfloat16)
        grad_one_ref[rows, :] = low
        return carry + fold(low.astype(jnp.float32))

    zeros = jnp.zeros((8, channels), jnp.float32)
    sums_ref[4:5, :] = column_total(each_chunk(pixels, finish, zeros))
    weight_part(
        act_one_ref, grad_one_ref, mask_ref, narrow_ref, columns_ref, part_ref, part_refs, cols
    )


def first_kernel(
    grad_one_ref,
    features_ref,
    residual_grad_ref,
    table_ref,
    mask_ref,
    old_sums_ref,
    weights_hbm,
    input_grad_ref,
    sums_ref,
    weights_ref,
    taps_ref,
    total_ref,
    sem,
    *,
    cols,
):
    copy = pltpu.make_async_copy(weights_hbm.at[0], weights_ref, sem)
    copy.start()
    sums, back = conv_back(
        grad_one_ref,
        copy,
        weights_ref,
        mask_ref,
        taps_ref,
        total_ref,
        lambda rows: features_ref[rows, :].astype(jnp.float32),
        table_ref,
        0,
        cols,
    )
    sums_ref[...] = old_sums_ref[...]
    sums_ref[0:1, :] = column_total(sums[1])
    sums_ref[1:2, :] = column_total(sums[0])
    count = input_grad_ref.shape[0]
    own = pl.ds(pl.multiple_of(lax.axis_index("height") * count, count), count)
    input_grad_ref[...] = (residual_grad_ref[own, :] + back(own)).astype(jnp.bfloat16)


def blend_kernel(*refs):
    count = len(refs) // 3
    mixed, parts, joints = refs[:count], refs[count : 2 * count], refs[2 * count :]
    total = mixed[0][...].astype(jnp.float32)
    for piece in mixed[1:]:
        total = total + piece[...].astype(jnp.float32)
    total = total.astype(jnp.bfloat16)
    share, width = total.shape
    for part, joint in zip(parts, joints):
        for block in range(width // LANES):
            joint[block * share : (block + 1) * share, :] = total[
                :, block * LANES : (block + 1) * LANES
            ]
        joint[width // LANES * share :, :] = part[...]


def place_kernel(*refs):
    joints, (qkv_hbm, proj_hbm, packed_ref, qkv_ref, proj_ref, sems) = refs[:-6], refs[-6:]
    half, width = packed_ref.shape
    share = half // len(joints)
    me = lax.axis_index("canvas")
    for step, joint in enumerate(joints):
        place = pl.ds(pl.multiple_of((me ^ step) * share, share), share)
        for block in range(width // LANES):
            packed_ref[place, block * LANES : (block + 1) * LANES] = joint[
                block * share : (block + 1) * share, :
            ]
    core = lax.axis_index("height") & 1
    spread_half(core, packed_ref, qkv_ref, proj_ref, qkv_hbm, proj_hbm, sems)


def spread_half(owner, packed_ref, qkv_ref, proj_ref, qkv_hbm, proj_hbm, sems):
    half = packed_ref.shape[0]
    inner = qkv_ref.shape[1]
    rows = pl.ds(pl.multiple_of(owner * half, half), half)
    qkv_ref[...] = packed_ref[:, 0:inner].astype(jnp.float32)
    copies = [pltpu.make_async_copy(qkv_ref, qkv_hbm.at[rows, :], sems.at[0])]
    copies[0].start()
    proj_ref[...] = packed_ref[:, inner:].astype(jnp.float32)
    copies.append(pltpu.make_async_copy(proj_ref, proj_hbm.at[rows, :], sems.at[1]))
    copies[1].start()
    for copy in copies:
        copy.wait()


def join_kernel(*refs):
    ins, (qkv_hbm, proj_hbm, conv_ref, qkv_ref, proj_ref, sems) = refs[:-6], refs[-6:]
    packed_ref, parts = ins[2], ins[3:]
    count = len(parts) // 2
    rows = parts[0].shape[0]
    for which in range(2):
        total = jnp.zeros(parts[0].shape, jnp.float32)
        for part in parts[which * count : (which + 1) * count]:
            total = total + part[part.shape[0] - rows :, :].astype(jnp.float32)
        conv_ref[which] = total.reshape(conv_ref.shape[1:])
    core = lax.axis_index("height") & 1
    spread_half(1 - core, packed_ref, qkv_ref, proj_ref, qkv_hbm, proj_hbm, sems)


def sums_kernel(*refs):
    gains_ref, shifts_ref, conv_ref, qv_ref, proj_ref = refs[-5:]
    total = refs[0][...]
    for ref in refs[1:-5]:
        total = total + ref[...]
    for row, start in enumerate((0, 2, 5)):
        gains_ref[row : row + 1, :] = total[start : start + 1]
        shifts_ref[row : row + 1, :] = total[start + 1 : start + 2]
    conv_ref[0:1, :] = total[4:5]
    conv_ref[1:2, :] = total[7:8]
    qv_ref[...] = total[8:10]
    proj_ref[...] = total[10:11]


def call_kernel(kernel, outputs, scratch, operands, places, flops, limit, out_places=None, aliases={}):
    out_places = out_places or "v" * len(outputs)
    spaces = {
        "v": pl.BlockSpec(memory_space=pltpu.VMEM),
        "s": pl.BlockSpec(memory_space=pltpu.SMEM),
        "h": pl.BlockSpec(memory_space=pl.ANY),
        "o": pl.BlockSpec(memory_space=pltpu.VMEM),
        "a": pl.BlockSpec(memory_space=pl.ANY),
    }
    moved = sum(array.size * array.dtype.itemsize for array in operands)
    held = {"v": pltpu.VMEM, "h": pltpu.HBM, "o": jax.ShapeDtypeStruct}
    operands = [
        pltpu.with_memory_space_constraint(array, pltpu.HBM) if place == "h" else array
        for array, place in zip(operands, places)
    ]
    return pl.pallas_call(
        kernel,
        out_shape=[held[place](*output) for output, place in zip(outputs, out_places)],
        in_specs=[spaces[place] for place in places],
        out_specs=[spaces[place] for place in out_places],
        scratch_shapes=scratch,
        input_output_aliases=aliases,
        compiler_params=pltpu.CompilerParams(vmem_limit_bytes=limit * 2**20),
        cost_estimate=pl.CostEstimate(flops=flops, bytes_accessed=moved, transcendentals=0),
    )(*operands)


def send_height(block, step):
    size = lax.axis_size("height")
    return lax.ppermute(block, "height", [(i, i ^ step) for i in range(size)])


def send_chips(block):
    return [send_height(block, step) for step in range(2, lax.axis_size("height"), 2)]


def with_cores(blocks):
    return [piece for block in blocks for piece in (block, send_height(block, 1))]


def trade_canvas(pieces):
    size = lax.axis_size("canvas")
    return [pieces[0]] + [
        lax.ppermute(piece, "canvas", [(i, i ^ step) for i in range(size)])
        for step, piece in enumerate(pieces)
        if step
    ]


def whole_canvas(
    features,
    tile_ids,
    norm_gains,
    norm_shifts,
    conv_weights,
    conv_biases,
    qkv_weight,
    qv_bias,
    proj_weight,
    proj_bias,
    cotangent,
):
    height_size = lax.axis_size("height")
    canvas_size = lax.axis_size("canvas")
    local_rows, cols, channels = features.shape[1:]
    all_rows = tile_ids.shape[1]
    pixels = all_rows * cols
    own_pixels = local_rows * cols
    out_share = channels // height_size
    ci_share = channels // canvas_size
    row_share = channels // 2 // canvas_size
    low, wide = jnp.bfloat16, jnp.float32

    own_features = features.reshape(own_pixels, channels)
    own_grad = cotangent.reshape(own_pixels, channels)
    held_features = [own_features] + send_chips(own_features)
    pieces = with_cores(held_features)
    own_grad, *pieces[::2] = lax.optimization_barrier((own_grad, *held_features))
    held_grads = [own_grad] + send_chips(own_grad)

    plane = ((pixels, channels), low)
    plane_wide = ((pixels, channels), wide)
    sums_shape = ((16, channels), wide)
    part_shapes = [((9 * out_share, ci_share), low)] * canvas_size
    mixed_shapes = [((row_share, 4 * channels), low)] * canvas_size
    taps = pltpu.VMEM((pixels + 2 * cols, 3 * channels), low)
    held = pltpu.VMEM((pixels, channels), low)
    held_wide = pltpu.VMEM((pixels, channels), wide)
    flipped = pltpu.VMEM((channels, pixels), low)
    half_flipped = pltpu.VMEM((channels // 2, pixels), low)
    half_mixed = pltpu.VMEM((channels // 2, 4 * channels), low)
    half_qkv = pltpu.VMEM((channels // 2, 3 * channels), wide)
    half_proj = pltpu.VMEM((channels // 2, channels), wide)
    conv_held = pltpu.VMEM(conv_weights.shape[1:], low)
    narrow = pltpu.VMEM((pixels + 2 * cols, 3 * NARROW), wide)
    columns = pltpu.VMEM((pixels, 5 * NARROW), low)
    part_held = pltpu.VMEM((5 * NARROW, channels), low)
    sem = pltpu.SemaphoreType.DMA
    conv_flops = 2 * 9 * pixels * channels * channels
    dot_flops = 2 * pixels * channels * channels
    score_flops = 2 * pixels * pixels * channels
    scale = channels ** (-0.5)

    (
        all_features,
        act_one,
        middle,
        act_two,
        residual,
        table,
        mask,
        id_rows,
        id_cols,
    ) = call_kernel(
        functools.partial(conv_kernel, cols=cols, count=height_size),
        [
            plane,
            plane,
            plane_wide,
            plane,
            plane_wide,
            ((16, channels), wide),
            ((2, pixels, LANES), wide),
            ((pixels, LANES), jnp.int32),
            ((8, pixels), jnp.int32),
        ],
        [
            pltpu.SMEM(tile_ids.shape, jnp.int32),
            pltpu.VMEM(norm_gains.shape, wide),
            pltpu.VMEM(norm_shifts.shape, wide),
            pltpu.VMEM(conv_biases.shape, wide),
            pltpu.VMEM(conv_weights.shape, low),
            taps,
            sem((6,)),
            sem((height_size,)),
        ],
        [*pieces, tile_ids, norm_gains, norm_shifts, conv_biases, conv_weights],
        "h" + "a" * (height_size - 1) + "h" * 5,
        2 * conv_flops,
        20,
    )
    residual, *held_grads = lax.optimization_barrier((residual, *held_grads))
    grad_pieces = with_cores(held_grads)
    normed, query, key, value, soft, out_flip, output = call_kernel(
        functools.partial(score_kernel, score_scale=scale),
        [
            plane,
            plane,
            plane,
            plane,
            ((pixels, pixels), low),
            ((channels, pixels), low),
            ((own_pixels, channels), low),
        ],
        [
            pltpu.VMEM(qkv_weight.shape, low),
            pltpu.VMEM(qv_bias.shape, wide),
            pltpu.VMEM(proj_weight.shape, low),
            pltpu.VMEM((1, channels), wide),
            flipped,
            sem((4,)),
        ],
        [
            qkv_weight,
            qv_bias,
            proj_weight,
            proj_bias.reshape(1, channels),
            residual,
            table,
            id_rows,
            id_cols,
        ],
        "hhhhvvvv",
        3 * dot_flops + 2 * score_flops,
        16,
        "v" * 6 + "o",
    )
    normed, *grad_pieces = lax.optimization_barrier((normed, *grad_pieces))
    all_grad, packed, sums, *mixed = call_kernel(
        functools.partial(attention_kernel, score_scale=scale, count=height_size),
        [plane, ((pixels, 3 * channels), low), sums_shape, *mixed_shapes],
        [
            half_mixed,
            pltpu.VMEM(proj_weight.shape, low),
            flipped,
            held_wide,
            held_wide,
            half_flipped,
            sem((height_size + 1,)),
        ],
        [proj_weight, normed, query, key, value, soft, out_flip, *grad_pieces],
        "hvvvvvvh" + "a" * (height_size - 1),
        3 * dot_flops + 4 * score_flops,
        20,
    )
    mixed = trade_canvas(mixed)
    residual_grad, grad_two, sums, *parts_two = call_kernel(
        functools.partial(third_kernel, cols=cols),
        [plane_wide, plane, sums_shape, *part_shapes],
        [
            pltpu.VMEM(qkv_weight.shape, low),
            held_wide,
            narrow,
            columns,
            part_held,
            sem,
        ],
        [qkv_weight, all_grad, packed, residual, table, act_two, mask, sums],
        "hvvvvvvv",
        3 * dot_flops + conv_flops // height_size,
        16,
    )
    joint_shape = (row_share * 4 * channels // LANES + 9 * out_share, LANES)
    joints = call_kernel(
        blend_kernel, [(joint_shape, low)] * canvas_size, [], mixed + parts_two, "v" * 2 * canvas_size, 0, 12
    )
    joints = trade_canvas(joints)
    back_scratch = [conv_held, taps, held_wide]
    grad_one, sums, *parts_one = call_kernel(
        functools.partial(second_kernel, cols=cols),
        [plane, sums_shape, *part_shapes],
        back_scratch + [narrow, columns, part_held, sem],
        [grad_two, middle, table, act_one, mask, sums, conv_weights],
        "vvvvvvh",
        conv_flops + conv_flops // height_size,
        24,
    )
    parts_one = trade_canvas(parts_one)
    *joints, grad_one = lax.optimization_barrier((*joints, grad_one))
    qkv_grad, proj_grad, mixed_half = call_kernel(
        place_kernel,
        [(qkv_weight.shape, wide), (proj_weight.shape, wide), ((channels // 2, 4 * channels), low)],
        [half_qkv, half_proj, sem((2,))],
        joints,
        "v" * canvas_size,
        0,
        12,
        "hhv",
    )
    mixed_other = lax.ppermute(mixed_half, "height", [(i, i ^ 1) for i in range(height_size)])
    input_grad, sums = call_kernel(
        functools.partial(first_kernel, cols=cols),
        [((own_pixels, channels), low), sums_shape],
        back_scratch + [sem],
        [grad_one, all_features, residual_grad, table, mask, sums, conv_weights],
        "vvvvvvh",
        conv_flops,
        20,
        "ov",
    )
    sums, mixed_other, *parts_one = lax.optimization_barrier((sums, mixed_other, *parts_one))
    all_sums = trade_canvas([sums] * canvas_size)
    qkv_grad, proj_grad, conv_grad = call_kernel(
        join_kernel,
        [
            (qkv_weight.shape, wide),
            (proj_weight.shape, wide),
            ((2, 3, 3, out_share, ci_share), wide),
        ],
        [half_qkv, half_proj, sem((2,))],
        [qkv_grad, proj_grad, mixed_other, *parts_one, *joints],
        "hhv" + "v" * (2 * canvas_size),
        0,
        12,
        "hho",
        {0: 0, 1: 1},
    )
    vector_shapes = [norm_gains.shape, norm_shifts.shape, conv_biases.shape, qv_bias.shape]
    gains_grad, shifts_grad, biases_grad, qv_grad, proj_bias_grad = call_kernel(
        sums_kernel,
        [(shape, wide) for shape in vector_shapes + [(1, channels)]],
        [],
        all_sums,
        "v" * canvas_size,
        0,
        16,
        "ooooo",
    )
    own_shape = (1, local_rows, cols, channels)
    return (
        output.reshape(own_shape),
        input_grad.reshape(own_shape),
        gains_grad,
        shifts_grad,
        jnp.swapaxes(conv_grad, 3, 4),
        biases_grad,
        qkv_grad,
        qv_grad,
        proj_grad,
        proj_bias_grad.reshape(channels),
    )


def on_device(*arrays):
    features, tile_ids = arrays[0], arrays[1]
    local_rows, cols, channels = features.shape[1:]
    pixels = tile_ids.shape[1] * cols
    height_size, canvas_size = lax.axis_size("height"), lax.axis_size("canvas")
    powers = all(size & (size - 1) == 0 for size in (height_size, canvas_size, cols))
    fits = (
        powers
        and height_size > 1
        and channels == LANES * canvas_size
        and pixels <= MOST_PIXELS
        and pixels % CONV_ROWS == 0
        and (local_rows * cols) % LANES == 0
        and CHUNK % cols == 0
        and cols % 16 == 0
        and channels % (LANES * canvas_size) == 0
        and 2 * channels == NARROW * height_size
    )
    return whole_canvas(*arrays) if fits else split_canvas(*arrays)


def solution(mesh):
    in_specs = (
        P("canvas", "height", None, None),
        P("canvas", None),
        P(),
        P(),
        P(),
        P(),
        P(),
        P(),
        P(),
        P(),
        P("canvas", "height", None, None),
    )
    out_specs = (
        P("canvas", "height", None, None),
        P("canvas", "height", None, None),
        P(),
        P(),
        P(None, None, None, "canvas", "height"),
        P(),
        P(),
        P(),
        P(),
        P(),
    )
    return jax.shard_map(
        on_device, mesh=mesh, in_specs=in_specs, out_specs=out_specs, check_vma=False
    )
```

```python
import functools

import jax
import jax.numpy as jnp
from jax import lax
from jax.experimental import pallas as pl
from jax.experimental.pallas import tpu as pltpu
from jax.sharding import PartitionSpec as P

GROUPS = 32


epsilon = 1e-06
masked_score = -1e30
MOST_PIXELS = 1024
LANES = 128
NARROW = 128
CHUNK = 128
CONV_ROWS = 1024
QUERY_ROWS = 512


def extended(block, sides, width):
    for axis, dim in sides:
        count = lax.axis_size(axis)
        forward = [(i, i + 1) for i in range(count - 1)]
        backward = [(target, source) for source, target in forward]
        low = lax.ppermute(
            lax.slice_in_dim(block, block.shape[dim] - width, None, axis=dim), axis, forward
        )
        high = lax.ppermute(lax.slice_in_dim(block, 0, width, axis=dim), axis, backward)
        block = jnp.concatenate([low, block, high], axis=dim)
    return block


def group_total(vector):
    return vector.reshape(GROUPS, -1).sum(axis=1)


def spread_groups(vector, channels):
    return jnp.repeat(vector, channels // GROUPS)


def norm_forward(values, gain, shift, members):
    channels = values.shape[1]
    totals = lax.psum(group_total(jnp.sum(values, axis=0)), "height")
    centered = values - spread_groups(totals / members, channels)
    squares = lax.psum(group_total(jnp.sum(centered * centered, axis=0)), "height")
    inverse = spread_groups(lax.rsqrt(squares / members + epsilon), channels)
    normed = centered * inverse
    return (normed, inverse, normed * gain + shift)


def norm_backward(grad_in, normed, inverse, gain, members):
    channels = grad_in.shape[1]
    scaled = grad_in * gain
    both_sums = lax.psum(
        (group_total(jnp.sum(scaled, axis=0)), group_total(jnp.sum(scaled * normed, axis=0))),
        "height",
    )
    mean_grad = spread_groups(both_sums[0] / members, channels)
    mean_cross = spread_groups(both_sums[1] / members, channels)
    result = inverse * (scaled - mean_grad - normed * mean_cross)
    return (result, jnp.sum(grad_in * normed, axis=0), jnp.sum(grad_in, axis=0))


def swish(values):
    return values * jax.nn.sigmoid(values)


def swish_slope(values):
    sigmoid_part = jax.nn.sigmoid(values)
    return sigmoid_part * (1.0 + values * (1.0 - sigmoid_part))


def tap_columns(padded, row_mask, local_rows, canvas_cols):
    pieces = []
    for row_tap in range(3):
        rows_taken = padded[row_tap : row_tap + local_rows] * row_mask[:, row_tap, None, None]
        for col_tap in range(3):
            pieces.append(rows_taken[:, col_tap : col_tap + canvas_cols])
    stacked = jnp.concatenate(pieces, axis=2)
    return stacked.reshape(local_rows * canvas_cols, stacked.shape[2])


def conv_forward(acts, row_mask, weight, bias):
    local_rows, canvas_cols, channels = acts.shape
    rimmed = extended(acts, (("height", 0),), 1)
    padded = jnp.pad(rimmed, ((0, 0), (1, 1), (0, 0)))
    gathered = tap_columns(padded, row_mask, local_rows, canvas_cols)
    result = (
        jnp.dot(
            gathered, weight.reshape(9 * channels, channels), preferred_element_type=jnp.float32
        )
        + bias
    )
    return (result, gathered)


def conv_backward(grad_low, row_mask, weight, gathered):
    local_rows, canvas_cols, channels = grad_low.shape
    flat_grad = grad_low.reshape(local_rows * canvas_cols, channels)
    weight_grad = lax.dot_general(
        gathered, flat_grad, (((0,), (0,)), ((), ())), preferred_element_type=jnp.float32
    )
    rimmed = extended(grad_low, (("height", 0),), 1)
    padded = jnp.pad(rimmed, ((0, 0), (1, 1), (0, 0)))
    grad_taps = tap_columns(padded, row_mask, local_rows, canvas_cols)
    flipped = jnp.transpose(weight[::-1, ::-1], (0, 1, 3, 2)).reshape(9 * channels, channels)
    input_part = jnp.dot(grad_taps, flipped, preferred_element_type=jnp.float32)
    return (
        input_part,
        weight_grad.reshape(3, 3, channels, channels),
        jnp.sum(flat_grad.astype(jnp.float32), axis=0),
    )


def take_rows(array, offset, count):
    return lax.dynamic_slice_in_dim(array, offset, count)


def score_grads(
    queries, out_grad, log_total, row_dots, query_ids, key_rows, value_rows, key_ids, score_scale
):
    scores = (
        lax.dot_general(
            queries, key_rows, (((1,), (1,)), ((), ())), preferred_element_type=jnp.float32
        )
        * score_scale
    )
    same_tile = query_ids[:, None] == key_ids[None, :]
    softmax_block = jnp.exp(jnp.where(same_tile, scores - log_total[:, None], masked_score))
    weight_grad = lax.dot_general(
        out_grad, value_rows, (((1,), (1,)), ((), ())), preferred_element_type=jnp.float32
    )
    score_grad = (softmax_block * (weight_grad - row_dots[:, None])).astype(jnp.bfloat16)
    return (softmax_block.astype(jnp.bfloat16), score_grad)


def split_canvas(
    features,
    tile_ids,
    norm_gains,
    norm_shifts,
    conv_weights,
    conv_biases,
    qkv_weight,
    qv_bias,
    proj_weight,
    proj_bias,
    cotangent,
):
    height_size = lax.axis_size("height")
    local_rows = features.shape[1]
    canvas_cols = features.shape[2]
    channels = features.shape[3]
    pixels = local_rows * canvas_cols
    row_ids = tile_ids[0]
    all_rows = row_ids.shape[0]
    members = float(all_rows * canvas_cols * (channels // GROUPS))
    score_scale = channels ** (-0.5)
    first_row = lax.axis_index("height") * local_rows
    edge_ids = jnp.full((1,), -1, jnp.int32)
    padded_ids = jnp.concatenate([edge_ids, row_ids, edge_ids])
    near_ids = lax.dynamic_slice_in_dim(padded_ids, first_row, local_rows + 2)
    own_rows = near_ids[1 : local_rows + 1]
    row_mask = jnp.stack(
        [near_ids[row_tap : row_tap + local_rows] == own_rows for row_tap in range(3)], axis=1
    ).astype(jnp.bfloat16)
    key_ids = jnp.repeat(row_ids, canvas_cols)
    query_ids = jnp.repeat(own_rows, canvas_cols)
    grid_shape = (local_rows, canvas_cols, channels)
    inputs = features[0].reshape(pixels, channels).astype(jnp.float32)
    normed_one, inverse_one, pre_one = norm_forward(inputs, norm_gains[0], norm_shifts[0], members)
    act_one = swish(pre_one).astype(jnp.bfloat16).reshape(grid_shape)
    middle, taps_one = conv_forward(act_one, row_mask, conv_weights[0], conv_biases[0])
    normed_two, inverse_two, pre_two = norm_forward(middle, norm_gains[1], norm_shifts[1], members)
    act_two = swish(pre_two).astype(jnp.bfloat16).reshape(grid_shape)
    branch, taps_two = conv_forward(act_two, row_mask, conv_weights[1], conv_biases[1])
    residual = inputs + branch
    normed_three, inverse_three, pre_three = norm_forward(
        residual, norm_gains[2], norm_shifts[2], members
    )
    attn_input = pre_three.astype(jnp.bfloat16)
    mixed = jnp.dot(attn_input, qkv_weight, preferred_element_type=jnp.float32)
    queries = (mixed[:, :channels] + qv_bias[0]).astype(jnp.bfloat16)
    key_rows = mixed[:, channels : 2 * channels].astype(jnp.bfloat16)
    value_rows = (mixed[:, 2 * channels :] + qv_bias[1]).astype(jnp.bfloat16)
    running_max = jnp.full((pixels,), masked_score, jnp.float32)
    key_piece = lax.all_gather(key_rows, "height", axis=0, tiled=True)
    value_piece = lax.all_gather(value_rows, "height", axis=0, tiled=True)
    scores = (
        lax.dot_general(
            queries, key_piece, (((1,), (1,)), ((), ())), preferred_element_type=jnp.float32
        )
        * score_scale
    )
    same_tile = query_ids[:, None] == key_ids[None, :]
    scores = jnp.where(same_tile, scores, masked_score)
    new_max = jnp.maximum(running_max, jnp.max(scores, axis=1))
    weights = jnp.where(same_tile, jnp.exp(scores - new_max[:, None]), 0.0)
    summed_out = jnp.dot(
        weights.astype(jnp.bfloat16), value_piece, preferred_element_type=jnp.float32
    )
    total_weight = jnp.sum(weights, axis=1)
    log_total = new_max + jnp.log(total_weight)
    attended = summed_out / total_weight[:, None]
    attended_low = attended.astype(jnp.bfloat16)
    output = (
        residual
        + jnp.dot(attended_low, proj_weight, preferred_element_type=jnp.float32)
        + proj_bias
    )
    out_grad = cotangent[0].reshape(pixels, channels)
    out_grad_full = out_grad.astype(jnp.float32)
    proj_grad = lax.dot_general(
        attended_low, out_grad, (((0,), (0,)), ((), ())), preferred_element_type=jnp.float32
    )
    proj_bias_grad = jnp.sum(out_grad_full, axis=0)
    attended_grad = lax.dot_general(
        out_grad, proj_weight, (((1,), (1,)), ((), ())), preferred_element_type=jnp.float32
    ).astype(jnp.bfloat16)
    row_dots = jnp.sum(attended_grad.astype(jnp.float32) * attended, axis=1)
    block_rows = pixels * min(height_size, 8)
    zero_block = jnp.zeros((pixels, channels), jnp.float32)
    key_all, value_all = (
        lax.all_gather(key_rows, "height", axis=0, tiled=True),
        lax.all_gather(value_rows, "height", axis=0, tiled=True),
    )
    query_all, grad_all = (
        lax.all_gather(queries, "height", axis=0, tiled=True),
        lax.all_gather(attended_grad, "height", axis=0, tiled=True),
    )
    total_all, dots_all = (
        lax.all_gather(log_total, "height", axis=0, tiled=True),
        lax.all_gather(row_dots, "height", axis=0, tiled=True),
    )

    def own_query_step(running, block_index):
        offset = block_index * block_rows
        key_part = take_rows(key_all, offset, block_rows)
        rounded, score_grad = score_grads(
            queries,
            attended_grad,
            log_total,
            row_dots,
            query_ids,
            key_part,
            take_rows(value_all, offset, block_rows),
            take_rows(key_ids, offset, block_rows),
            score_scale,
        )
        return (
            running
            + jnp.dot(score_grad, key_part, preferred_element_type=jnp.float32) * score_scale,
            None,
        )

    def own_key_step(running, block_index):
        offset = block_index * block_rows
        query_part = take_rows(query_all, offset, block_rows)
        grad_part = take_rows(grad_all, offset, block_rows)
        rounded, score_grad = score_grads(
            query_part,
            grad_part,
            take_rows(total_all, offset, block_rows),
            take_rows(dots_all, offset, block_rows),
            take_rows(key_ids, offset, block_rows),
            key_rows,
            value_rows,
            query_ids,
            score_scale,
        )
        key_part = (
            lax.dot_general(
                score_grad, query_part, (((0,), (0,)), ((), ())), preferred_element_type=jnp.float32
            )
            * score_scale
        )
        value_part = lax.dot_general(
            rounded, grad_part, (((0,), (0,)), ((), ())), preferred_element_type=jnp.float32
        )
        return ((running[0] + key_part, running[1] + value_part), None)

    block_count = key_all.shape[0] // block_rows
    query_grad, unused_one = lax.scan(own_query_step, zero_block, jnp.arange(block_count))
    (key_grad, value_grad), unused_two = lax.scan(
        own_key_step, (zero_block, zero_block), jnp.arange(block_count)
    )
    query_low = query_grad.astype(jnp.bfloat16)
    key_low = key_grad.astype(jnp.bfloat16)
    value_low = value_grad.astype(jnp.bfloat16)
    stacked_grad = jnp.concatenate([query_low, key_low, value_low], axis=1)
    qkv_grad = lax.dot_general(
        attn_input, stacked_grad, (((0,), (0,)), ((), ())), preferred_element_type=jnp.float32
    )
    qv_grad = jnp.stack(
        [
            jnp.sum(query_low.astype(jnp.float32), axis=0),
            jnp.sum(value_low.astype(jnp.float32), axis=0),
        ]
    )
    normed_grad = lax.dot_general(
        stacked_grad, qkv_weight, (((1,), (1,)), ((), ())), preferred_element_type=jnp.float32
    )
    back_three, gain_three, shift_three = norm_backward(
        normed_grad, normed_three, inverse_three, norm_gains[2], members
    )
    residual_grad = out_grad_full + back_three
    grad_two = residual_grad.astype(jnp.bfloat16).reshape(grid_shape)
    act_two_grad, weight_two_grad, bias_two_grad = conv_backward(
        grad_two, row_mask, conv_weights[1], taps_two
    )
    middle_grad, gain_two, shift_two = norm_backward(
        act_two_grad * swish_slope(pre_two), normed_two, inverse_two, norm_gains[1], members
    )
    grad_one = middle_grad.astype(jnp.bfloat16).reshape(grid_shape)
    act_one_grad, weight_one_grad, bias_one_grad = conv_backward(
        grad_one, row_mask, conv_weights[0], taps_one
    )
    input_back, gain_one, shift_one = norm_backward(
        act_one_grad * swish_slope(pre_one), normed_one, inverse_one, norm_gains[0], members
    )
    input_grad = residual_grad + input_back
    conv_grad = jnp.stack([weight_one_grad, weight_two_grad])
    conv_part = lax.psum_scatter(conv_grad, "height", scatter_dimension=4, tiled=True)
    conv_part = lax.psum_scatter(
        conv_part.astype(jnp.bfloat16), "canvas", scatter_dimension=3, tiled=True
    ).astype(jnp.float32)
    summed = lax.psum(
        (
            jnp.stack([gain_one, gain_two, gain_three]),
            jnp.stack([shift_one, shift_two, shift_three]),
            jnp.stack([bias_one_grad, bias_two_grad]),
            qkv_grad,
            qv_grad,
            proj_grad,
            proj_bias_grad,
        ),
        ("canvas", "height"),
    )
    return (
        output.astype(jnp.bfloat16).reshape((1,) + grid_shape),
        input_grad.astype(jnp.bfloat16).reshape((1,) + grid_shape),
        summed[0],
        summed[1],
        conv_part,
        summed[2],
        summed[3],
        summed[4],
        summed[5],
        summed[6],
    )


def fold(block):
    rows, width = block.shape
    return jnp.sum(block.reshape(rows // 8, 8, width), axis=0)


def group_lanes(block, group):
    lane = lax.broadcasted_iota(jnp.int32, block.shape, 1)
    width = block.shape[1]
    step = 1
    while step < group:
        above = pltpu.roll(block, step, 1)
        below = pltpu.roll(block, width - step, 1)
        block = block + jnp.where((lane & step) != 0, above, below)
        step *= 2
    return block


def group_mean(partial, members):
    spread = group_lanes(partial, partial.shape[1] // GROUPS)
    return jnp.sum(spread, axis=0, keepdims=True) * (1.0 / members)


def widen(block, width):
    return jnp.concatenate([block] * (width // block.shape[1]), axis=1)


def each_chunk(pixels, body, carry):
    def step(index, carry):
        return body(pl.ds(pl.multiple_of(index * CHUNK, CHUNK), CHUNK), carry)

    return lax.fori_loop(0, pixels // CHUNK, step, carry)


def norm_stats(read, pixels, channels):
    members = float(pixels * (channels // GROUPS))
    zeros = jnp.zeros((8, channels), jnp.float32)
    total = each_chunk(pixels, lambda rows, carry: carry + fold(read(rows)), zeros)
    mean = group_mean(total, members)

    def squares(rows, carry):
        centered = read(rows) - mean
        return carry + fold(centered * centered)

    spread = group_mean(each_chunk(pixels, squares, zeros), members)
    return mean, lax.rsqrt(spread + epsilon)


def put_taps(taps_ref, block, rows, cols):
    count, channels = block.shape
    place = lax.broadcasted_iota(jnp.int32, block.shape, 0) & (cols - 1)
    left = jnp.where(place == 0, 0.0, pltpu.roll(block, 1, 0))
    right = jnp.where(place == cols - 1, 0.0, pltpu.roll(block, count - 1, 0))
    inner = pl.ds(pl.multiple_of(rows.start + cols, cols), count)
    taps_ref[inner, 0:channels] = left.astype(jnp.bfloat16)
    taps_ref[inner, channels : 2 * channels] = block.astype(jnp.bfloat16)
    taps_ref[inner, 2 * channels :] = right.astype(jnp.bfloat16)


def clear_edges(taps_ref, cols):
    edge = jnp.zeros((cols, taps_ref.shape[1]), taps_ref.dtype)
    taps_ref[0:cols, :] = edge
    taps_ref[taps_ref.shape[0] - cols :, :] = edge


def run_conv(taps_ref, product, mask_ref, total_ref, first, cols):
    pixels, channels = total_ref.shape
    block = min(CONV_ROWS, pixels)
    for row_tap in (1, 0, 2):

        def step(index, carry):
            start = pl.multiple_of(index * block, block)
            rows = pl.ds(start, block)
            shifted = pl.ds(pl.multiple_of(start + row_tap * cols, cols), block)
            part = product(taps_ref, shifted, row_tap)
            if row_tap == 1:
                total_ref[rows, :] = first(rows) + part
            else:
                total_ref[rows, :] += widen(mask_ref[row_tap // 2, rows, :], channels) * part
            return carry

        lax.fori_loop(0, pixels // block, step, 0)


def product_forward(weight_ref):
    channels = weight_ref.shape[-1]

    def product(taps_ref, shifted, row_tap):
        return jnp.dot(
            taps_ref[shifted, :],
            weight_ref[row_tap].reshape(3 * channels, channels),
            preferred_element_type=jnp.float32,
        )

    return product


def product_backward(weight_ref):
    def product(taps_ref, shifted, row_tap):
        return lax.dot_general(
            taps_ref[shifted, :],
            weight_ref[row_tap],
            (((1,), (1,)), ((), ())),
            preferred_element_type=jnp.float32,
        )

    return product


def smooth(values):
    part = 0.5 * jnp.tanh(0.5 * values) + 0.5
    return values * part, part


def activate(read, mean, inverse, gain, shift, act_ref, taps_ref, cols):
    scale = inverse * gain

    def step(rows, carry):
        act = smooth((read(rows) - mean) * scale + shift)[0]
        act_ref[rows, :] = act.astype(jnp.bfloat16)
        put_taps(taps_ref, act, rows, cols)
        return carry

    each_chunk(act_ref.shape[0], step, 0)


def back_sums(read_pair, pixels, channels):
    zeros = jnp.zeros((8, channels), jnp.float32)

    def step(rows, carry):
        grad, normed = read_pair(rows)
        return carry[0] + fold(grad), carry[1] + fold(grad * normed)

    plain, cross = each_chunk(pixels, step, (zeros, zeros))
    return plain, cross


def back_means(sums, gain, pixels):
    channels = gain.shape[1]
    members = float(pixels * (channels // GROUPS))
    return group_mean(sums[0] * gain, members), group_mean(sums[1] * gain, members)


def column_total(partial):
    return jnp.sum(partial, axis=0, keepdims=True)


def weight_part(act_ref, grad_ref, mask_ref, narrow_ref, columns_ref, part_ref, cols):
    pixels, channels = act_ref.shape
    height = lax.axis_index("height")
    share = NARROW // 2
    block = pl.ds(pl.multiple_of((height // 2) * NARROW, NARROW), NARROW)
    parity = height % 2
    edge = jnp.zeros((cols, 3 * NARROW), jnp.float32)
    narrow_ref[0:cols, :] = edge
    narrow_ref[cols + pixels :, :] = edge

    def spread(rows, carry):
        own = grad_ref[rows, block].astype(jnp.float32)
        half = lax.broadcasted_iota(jnp.int32, own.shape, 1) // share
        turned = pltpu.roll(own, share, 1)
        both = jnp.where(half == parity, own, turned)
        place = lax.broadcasted_iota(jnp.int32, own.shape, 0) & (cols - 1)
        left = jnp.where(place == 0, 0.0, pltpu.roll(both, 1, 0))
        right = jnp.where(place == cols - 1, 0.0, pltpu.roll(both, CHUNK - 1, 0))
        inner = pl.ds(pl.multiple_of(rows.start + cols, cols), CHUNK)
        narrow_ref[inner, 0:NARROW] = left
        narrow_ref[inner, NARROW : 2 * NARROW] = both
        narrow_ref[inner, 2 * NARROW :] = right
        return carry

    each_chunk(pixels, spread, 0)

    def gather(rows, carry):
        taps = []
        for row_tap in range(3):
            for col_tap in range(3):
                row_back, col_back = 2 - row_tap, 2 - col_tap
                shifted = pl.ds(pl.multiple_of(rows.start + row_back * cols, cols), CHUNK)
                block = narrow_ref[shifted, col_back * NARROW : (col_back + 1) * NARROW]
                if row_back != 1:
                    block = block * mask_ref[row_back // 2, rows, :]
                taps.append(block)
        lower = lax.broadcasted_iota(jnp.int32, taps[0].shape, 1) < share
        for pair in range(5):
            second = taps[min(2 * pair + 1, 8)]
            columns_ref[rows, pair * NARROW : (pair + 1) * NARROW] = jnp.where(
                lower, taps[2 * pair], second
            ).astype(jnp.bfloat16)
        return carry

    each_chunk(pixels, gather, 0)
    part_ref[...] = lax.dot_general(
        columns_ref[...],
        act_ref[...],
        (((0,), (0,)), ((), ())),
        preferred_element_type=jnp.float32,
    ).astype(jnp.bfloat16)


def conv_back(grad_ref, weights_ref, mask_ref, taps_ref, total_ref, cols):
    clear_edges(taps_ref, cols)

    def spread(rows, carry):
        put_taps(taps_ref, grad_ref[rows, :].astype(jnp.float32), rows, cols)
        return carry

    each_chunk(grad_ref.shape[0], spread, 0)
    run_conv(
        taps_ref, product_backward(weights_ref), mask_ref, total_ref, lambda rows: 0.0, cols
    )


def norm_back(total_ref, slope_ref, read, table_ref, which):
    pixels, channels = total_ref.shape
    mean, inverse, gain, shift = norm_rows(table_ref, which)

    def slope(rows):
        normed = (read(rows) - mean) * inverse
        pre = normed * gain + shift
        part = smooth(pre)[1]
        grad = total_ref[rows, :] * (part * (1.0 + pre * (1.0 - part)))
        slope_ref[rows, :] = grad
        return grad, normed

    sums = back_sums(slope, pixels, channels)
    mean_grad, mean_cross = back_means(sums, gain, pixels)

    def back(rows):
        normed = (read(rows) - mean) * inverse
        return inverse * (slope_ref[rows, :] * gain - mean_grad - normed * mean_cross)

    return sums, back


def turn_kernel(grad_ref, mask_ref, weights_ref, total_ref, taps_ref, *, cols):
    conv_back(grad_ref, weights_ref.at[1], mask_ref, taps_ref, total_ref, cols)


def norm_rows(table_ref, which):
    picks = (2 * which, 2 * which + 1, 6 + which, 9 + which)
    return tuple(table_ref[pick : pick + 1, :] for pick in picks)


def build_masks(ids_ref, mask_ref, id_rows_ref, id_cols_ref, cols):
    rows = ids_ref.shape[1]
    for row in range(rows):
        here = ids_ref[0, row]
        place = slice(row * cols, (row + 1) * cols)
        id_rows_ref[place, :] = jnp.full((cols, LANES), here, jnp.int32)
        for side, other in ((0, row - 1), (1, row + 1)):
            same = jnp.float32(0.0)
            if 0 <= other < rows:
                same = jnp.where(ids_ref[0, other] == here, 1.0, 0.0).astype(jnp.float32)
            mask_ref[side, place, :] = jnp.full((cols, LANES), same, jnp.float32)
    lane = lax.broadcasted_iota(jnp.int32, (8, LANES), 1)
    each = LANES // cols
    for block in range(rows // each):
        ids = jnp.full((8, LANES), ids_ref[0, block * each], jnp.int32)
        for step in range(1, each):
            ids = jnp.where(lane >= step * cols, ids_ref[0, block * each + step], ids)
        id_cols_ref[:, block * LANES : (block + 1) * LANES] = ids


def place_pieces(pieces, whole_ref, sems):
    own_pixels = whole_ref.shape[0] // len(pieces)
    height = lax.axis_index("height")
    copies = []
    for place, piece in enumerate(pieces):
        start = pl.multiple_of((height ^ place) * own_pixels, own_pixels)
        rows = pl.ds(start, own_pixels)
        copies.append(pltpu.make_async_copy(piece, whole_ref.at[rows, :], sems.at[place]))
    return copies


def conv_kernel(*refs, cols, count):
    pieces, refs = refs[:count], refs[count:]
    (
        ids_hbm,
        gains_hbm,
        shifts_hbm,
        biases_hbm,
        weights_hbm,
        qkv_hbm,
        proj_hbm,
        features_ref,
        act_one_ref,
        middle_ref,
        act_two_ref,
        residual_ref,
        table_ref,
        mask_ref,
        id_rows_ref,
        id_cols_ref,
        turned_ref,
        qkv_ref,
        proj_ref,
        ids_ref,
        gains_ref,
        shifts_ref,
        biases_ref,
        weights_ref,
        taps_ref,
        sems,
        piece_sems,
    ) = refs
    pixels, channels = features_ref.shape
    wide = jnp.float32
    turned = [
        (
            weights_hbm.at[which, 2 - row_tap, 2 - col_tap],
            turned_ref.at[which, row_tap, :, col_tap * channels : (col_tap + 1) * channels],
        )
        for which in (1, 0)
        for row_tap in range(3)
        for col_tap in range(3)
    ]
    arrivals = place_pieces(pieces, features_ref, piece_sems)
    moves = [
        (ids_hbm, ids_ref),
        (gains_hbm, gains_ref),
        (shifts_hbm, shifts_ref),
        (weights_hbm.at[0], weights_ref.at[0]),
        (biases_hbm, biases_ref),
        (weights_hbm.at[1], weights_ref.at[1]),
        (qkv_hbm, qkv_ref),
        (proj_hbm, proj_ref),
    ] + turned
    copies = [
        pltpu.make_async_copy(source, target, sems.at[index])
        for index, (source, target) in enumerate(moves)
    ]
    for copy in copies[:1] + arrivals + copies[1:6]:
        copy.start()
    clear_edges(taps_ref, cols)
    copies[0].wait()
    build_masks(ids_ref, mask_ref, id_rows_ref, id_cols_ref, cols)
    for copy in arrivals:
        copy.wait()

    def read_input(rows):
        return features_ref[rows, :].astype(wide)

    def read_middle(rows):
        return middle_ref[rows, :]

    def read_residual(rows):
        return residual_ref[rows, :]

    table_ref[0:1, :], table_ref[1:2, :] = norm_stats(read_input, pixels, channels)
    copies[1].wait()
    copies[2].wait()
    table_ref[6:9, :] = gains_ref[...]
    table_ref[9:12, :] = shifts_ref[...]
    activate(read_input, *norm_rows(table_ref, 0), act_one_ref, taps_ref, cols)
    copies[3].wait()
    copies[4].wait()
    for copy in copies[6:]:
        copy.start()
    run_conv(
        taps_ref,
        product_forward(weights_ref.at[0]),
        mask_ref,
        middle_ref,
        lambda rows: biases_ref[0:1, :],
        cols,
    )
    table_ref[2:3, :], table_ref[3:4, :] = norm_stats(read_middle, pixels, channels)
    activate(read_middle, *norm_rows(table_ref, 1), act_two_ref, taps_ref, cols)
    copies[5].wait()
    run_conv(
        taps_ref,
        product_forward(weights_ref.at[1]),
        mask_ref,
        residual_ref,
        lambda rows: read_input(rows) + biases_ref[1:2, :],
        cols,
    )
    table_ref[4:5, :], table_ref[5:6, :] = norm_stats(read_residual, pixels, channels)
    for copy in copies[6:]:
        copy.wait()


def score_kernel(
    qv_bias_hbm,
    proj_bias_hbm,
    qkv_ref,
    proj_ref,
    residual_ref,
    table_ref,
    id_rows_ref,
    id_cols_ref,
    normed_ref,
    query_ref,
    key_ref,
    value_ref,
    soft_ref,
    out_flip_ref,
    output_ref,
    qv_bias_ref,
    proj_bias_ref,
    value_flip_ref,
    sems,
    *,
    score_scale,
):
    pixels, channels = residual_ref.shape
    own_pixels = output_ref.shape[0]
    wide = jnp.float32
    exponent = score_scale * 1.4426950408889634
    moves = [(qv_bias_hbm, qv_bias_ref), (proj_bias_hbm, proj_bias_ref)]
    copies = [
        pltpu.make_async_copy(source, target, sems.at[index])
        for index, (source, target) in enumerate(moves)
    ]
    for copy in copies:
        copy.start()
    mean, inverse, gain, shift = norm_rows(table_ref, 2)
    scale = inverse * gain
    for copy in copies:
        copy.wait()
    block = min(QUERY_ROWS, pixels)

    def project(index, carry):
        rows = pl.ds(pl.multiple_of(index * block, block), block)
        normed = ((residual_ref[rows, :] - mean) * scale + shift).astype(jnp.bfloat16)
        normed_ref[rows, :] = normed
        query_ref[rows, :] = (
            jnp.dot(normed, qkv_ref[:, 0:channels], preferred_element_type=wide)
            + qv_bias_ref[0:1, :]
        ).astype(jnp.bfloat16)
        key_ref[rows, :] = jnp.dot(
            normed, qkv_ref[:, channels : 2 * channels], preferred_element_type=wide
        ).astype(jnp.bfloat16)
        values = (
            jnp.dot(normed, qkv_ref[:, 2 * channels :], preferred_element_type=wide)
            + qv_bias_ref[1:2, :]
        ).astype(jnp.bfloat16)
        value_ref[rows, :] = values
        value_flip_ref[:, rows] = values.T
        return carry

    lax.fori_loop(0, pixels // block, project, 0)

    def attend(index, carry):
        rows = pl.ds(pl.multiple_of(index * block, block), block)
        scores = lax.dot_general(
            key_ref[...], query_ref[rows, :], (((1,), (1,)), ((), ())), preferred_element_type=wide
        )
        same = widen(id_rows_ref[...], block) == id_cols_ref[0:1, rows]
        scores = jnp.where(same, scores, masked_score)
        scores = jnp.exp2((scores - jnp.max(scores, axis=0, keepdims=True)) * exponent)
        weights = scores * (1.0 / jnp.sum(scores, axis=0, keepdims=True))
        rounded = weights.astype(jnp.bfloat16)
        soft_ref[:, rows] = rounded
        out_flip_ref[:, rows] = jnp.dot(
            value_flip_ref[...], rounded, preferred_element_type=wide
        ).astype(jnp.bfloat16)
        return carry

    lax.fori_loop(0, pixels // block, attend, 0)
    height = lax.axis_index("height")
    own = pl.ds(pl.multiple_of(height * own_pixels, own_pixels), own_pixels)
    output_ref[...] = (
        residual_ref[own, :]
        + lax.dot_general(
            out_flip_ref[:, own],
            proj_ref[...],
            (((0,), (0,)), ((), ())),
            preferred_element_type=wide,
        )
        + proj_bias_ref[...]
    ).astype(jnp.bfloat16)


def send_order(source_ref, targets, axis, share):
    me = lax.axis_index("canvas")
    for step, target in enumerate(targets):
        place = pl.ds(pl.multiple_of((me ^ step) * share, share), share)
        target[...] = source_ref[place, :] if axis == 0 else source_ref[:, place]


def attention_kernel(
    proj_ref,
    normed_ref,
    query_ref,
    key_ref,
    value_ref,
    soft_ref,
    out_flip_ref,
    *refs,
    score_scale,
    count,
):
    pieces, (grad_ref, packed_ref, sums_ref), refs = (
        refs[:count],
        refs[count : count + 3],
        refs[count + 3 :],
    )
    *mixed_refs, mixed_ref, key_flip_ref, key_sum_ref, value_sum_ref, flip_ref, sems = refs
    pixels, channels = normed_ref.shape
    block = min(QUERY_ROWS, pixels)
    wide = jnp.float32
    copies = place_pieces(pieces, grad_ref, sems)
    for copy in copies:
        copy.start()
    half = channels // 2
    core = lax.axis_index("height") & 1
    half_lanes = pl.ds(pl.multiple_of(core * half, half), half)
    flip_ref[...] = normed_ref[:, half_lanes].T
    key_flip_ref[...] = key_ref[...].T
    key_sum_ref[...] = jnp.zeros(key_sum_ref.shape, wide)
    value_sum_ref[...] = jnp.zeros(value_sum_ref.shape, wide)
    for copy in copies:
        copy.wait()

    def attend(index, carry):
        rows = pl.ds(pl.multiple_of(index * block, block), block)
        back = lax.dot_general(
            grad_ref[rows, :], proj_ref[...], (((1,), (1,)), ((), ())), preferred_element_type=wide
        ).astype(jnp.bfloat16)
        rounded = soft_ref[:, rows]
        weights = rounded.astype(wide)
        weight_grad = lax.dot_general(
            value_ref[...], back, (((1,), (1,)), ((), ())), preferred_element_type=wide
        )
        value_sum_ref[...] += jnp.dot(rounded, back, preferred_element_type=wide)
        dots = jnp.sum(weights * weight_grad, axis=0, keepdims=True)
        score_grad = (weights * (weight_grad - dots)).astype(jnp.bfloat16)
        key_sum_ref[...] += jnp.dot(score_grad, query_ref[rows, :], preferred_element_type=wide)
        query_grad = jnp.dot(key_flip_ref[...], score_grad, preferred_element_type=wide)
        packed_ref[rows, 0:channels] = (query_grad * score_scale).astype(jnp.bfloat16).T
        return carry

    lax.fori_loop(0, pixels // block, attend, 0)

    def pack(rows, carry):
        packed_ref[rows, channels : 2 * channels] = (key_sum_ref[rows, :] * score_scale).astype(
            jnp.bfloat16
        )
        packed_ref[rows, 2 * channels :] = value_sum_ref[rows, :].astype(jnp.bfloat16)
        return (
            carry[0] + fold(packed_ref[rows, 0:channels].astype(wide)),
            carry[1] + fold(packed_ref[rows, 2 * channels :].astype(wide)),
            carry[2] + fold(grad_ref[rows, :].astype(wide)),
        )

    zeros = jnp.zeros((8, channels), wide)
    totals = each_chunk(pixels, pack, (zeros, zeros, zeros))
    sums_ref[...] = jnp.zeros(sums_ref.shape, wide)
    for row, total in enumerate(totals):
        sums_ref[8 + row : 9 + row, :] = column_total(total)

    half_rows = pl.ds(pl.multiple_of(core * half, half), half)
    mixed_ref[:, 0 : 3 * channels] = jnp.dot(
        flip_ref[...], packed_ref[...], preferred_element_type=wide
    ).astype(jnp.bfloat16)
    mixed_ref[:, 3 * channels :] = jnp.dot(
        out_flip_ref[half_rows, :], grad_ref[...], preferred_element_type=wide
    ).astype(jnp.bfloat16)
    send_order(mixed_ref, mixed_refs, 0, half // len(mixed_refs))


def third_kernel(
    qkv_ref,
    grad_ref,
    packed_ref,
    residual_ref,
    table_ref,
    act_two_ref,
    mask_ref,
    old_sums_ref,
    residual_grad_ref,
    grad_two_ref,
    sums_ref,
    *refs,
    cols,
):
    *part_refs, total_ref, narrow_ref, columns_ref, part_ref = refs
    pixels, channels = residual_ref.shape
    block = min(CONV_ROWS, pixels)
    wide = jnp.float32
    mean, inverse, gain, shift = norm_rows(table_ref, 2)
    zeros = jnp.zeros((8, channels), wide)

    def input_grads(index, carry):
        rows = pl.ds(pl.multiple_of(index * block, block), block)
        normed_grad = lax.dot_general(
            packed_ref[rows, :], qkv_ref[...], (((1,), (1,)), ((), ())), preferred_element_type=wide
        )
        total_ref[rows, :] = normed_grad
        normed = (residual_ref[rows, :] - mean) * inverse
        return carry[0] + fold(normed_grad), carry[1] + fold(normed_grad * normed)

    sums = lax.fori_loop(0, pixels // block, input_grads, (zeros, zeros))
    sums_ref[...] = old_sums_ref[...]
    sums_ref[5:6, :] = column_total(sums[1])
    sums_ref[6:7, :] = column_total(sums[0])
    mean_grad, mean_cross = back_means(sums, gain, pixels)

    def finish(rows, carry):
        normed = (residual_ref[rows, :] - mean) * inverse
        back = inverse * (total_ref[rows, :] * gain - mean_grad - normed * mean_cross)
        total = grad_ref[rows, :].astype(wide) + back
        residual_grad_ref[rows, :] = total
        low = total.astype(jnp.bfloat16)
        grad_two_ref[rows, :] = low
        return carry + fold(low.astype(wide))

    sums_ref[7:8, :] = column_total(each_chunk(pixels, finish, zeros))
    weight_part(act_two_ref, grad_two_ref, mask_ref, narrow_ref, columns_ref, part_ref, cols)
    rows, width = part_refs[0].shape
    send_order(part_ref.at[0:rows, :], part_refs, 1, width)


def second_kernel(
    total_ref,
    middle_ref,
    table_ref,
    act_one_ref,
    mask_ref,
    old_sums_ref,
    grad_one_ref,
    sums_ref,
    parts_ref,
    slope_ref,
    narrow_ref,
    columns_ref,
    part_ref,
    *,
    cols,
):
    pixels, channels = middle_ref.shape
    sums, back = norm_back(total_ref, slope_ref, lambda rows: middle_ref[rows, :], table_ref, 1)
    sums_ref[...] = old_sums_ref[...]
    sums_ref[2:3, :] = column_total(sums[1])
    sums_ref[3:4, :] = column_total(sums[0])

    def finish(rows, carry):
        low = back(rows).astype(jnp.bfloat16)
        grad_one_ref[rows, :] = low
        return carry + fold(low.astype(jnp.float32))

    zeros = jnp.zeros((8, channels), jnp.float32)
    sums_ref[4:5, :] = column_total(each_chunk(pixels, finish, zeros))
    weight_part(act_one_ref, grad_one_ref, mask_ref, narrow_ref, columns_ref, part_ref, cols)
    rows, width = parts_ref.shape[1:]
    for piece in range(parts_ref.shape[0]):
        parts_ref[piece] = part_ref[0:rows, piece * width : (piece + 1) * width]


def first_kernel(
    grad_one_ref,
    features_ref,
    residual_grad_ref,
    table_ref,
    mask_ref,
    old_sums_ref,
    weights_ref,
    input_grad_ref,
    sums_ref,
    taps_ref,
    total_ref,
    *,
    cols,
):
    conv_back(grad_one_ref, weights_ref.at[0], mask_ref, taps_ref, total_ref, cols)
    sums, back = norm_back(
        total_ref,
        total_ref,
        lambda rows: features_ref[rows, :].astype(jnp.float32),
        table_ref,
        0,
    )
    sums_ref[...] = old_sums_ref[...]
    sums_ref[0:1, :] = column_total(sums[1])
    sums_ref[1:2, :] = column_total(sums[0])
    count = input_grad_ref.shape[0]
    own = pl.ds(pl.multiple_of(lax.axis_index("height") * count, count), count)
    input_grad_ref[...] = (residual_grad_ref[own, :] + back(own)).astype(jnp.bfloat16)


def blend_kernel(*refs):
    count = len(refs) // 3
    mixed, parts, joints = refs[:count], refs[count : 2 * count], refs[2 * count :]
    total = mixed[0][...].astype(jnp.float32)
    for piece in mixed[1:]:
        total = total + piece[...].astype(jnp.float32)
    total = total.astype(jnp.bfloat16)
    share, width = total.shape
    for part, joint in zip(parts, joints):
        for block in range(width // LANES):
            joint[block * share : (block + 1) * share, :] = total[
                :, block * LANES : (block + 1) * LANES
            ]
        joint[width // LANES * share :, :] = part[...]


def place_kernel(*refs):
    joints, (qkv_hbm, proj_hbm, packed_ref, qkv_ref, proj_ref, sems) = refs[:-6], refs[-6:]
    half, width = packed_ref.shape
    share = half // len(joints)
    me = lax.axis_index("canvas")
    for step, joint in enumerate(joints):
        place = pl.ds(pl.multiple_of((me ^ step) * share, share), share)
        for block in range(width // LANES):
            packed_ref[place, block * LANES : (block + 1) * LANES] = joint[
                block * share : (block + 1) * share, :
            ]
    core = lax.axis_index("height") & 1
    spread_half(core, packed_ref, qkv_ref, proj_ref, qkv_hbm, proj_hbm, sems)


def spread_half(owner, packed_ref, qkv_ref, proj_ref, qkv_hbm, proj_hbm, sems):
    half = packed_ref.shape[0]
    inner = qkv_ref.shape[1]
    rows = pl.ds(pl.multiple_of(owner * half, half), half)
    qkv_ref[...] = packed_ref[:, 0:inner].astype(jnp.float32)
    copies = [pltpu.make_async_copy(qkv_ref, qkv_hbm.at[rows, :], sems.at[0])]
    copies[0].start()
    proj_ref[...] = packed_ref[:, inner:].astype(jnp.float32)
    copies.append(pltpu.make_async_copy(proj_ref, proj_hbm.at[rows, :], sems.at[1]))
    copies[1].start()
    for copy in copies:
        copy.wait()


def join_kernel(*refs):
    ins, (qkv_hbm, proj_hbm, conv_ref, qkv_ref, proj_ref, sems) = refs[:-6], refs[-6:]
    packed_ref, ones_ref, joints = ins[2], ins[3], ins[4:]
    count, rows = ones_ref.shape[:2]
    ones = [ones_ref[piece] for piece in range(count)]
    twos = [joint[joint.shape[0] - rows :, :] for joint in joints]
    for which, parts in enumerate((ones, twos)):
        total = parts[0].astype(jnp.float32)
        for part in parts[1:]:
            total = total + part.astype(jnp.float32)
        conv_ref[which] = total.reshape(conv_ref.shape[1:])
    core = lax.axis_index("height") & 1
    spread_half(1 - core, packed_ref, qkv_ref, proj_ref, qkv_hbm, proj_hbm, sems)


def sums_kernel(*refs):
    gains_ref, shifts_ref, conv_ref, qv_ref, proj_ref = refs[-5:]
    total = refs[0][...]
    for ref in refs[1:-5]:
        total = total + ref[...]
    for row, start in enumerate((0, 2, 5)):
        gains_ref[row : row + 1, :] = total[start : start + 1]
        shifts_ref[row : row + 1, :] = total[start + 1 : start + 2]
    conv_ref[0:1, :] = total[4:5]
    conv_ref[1:2, :] = total[7:8]
    qv_ref[...] = total[8:10]
    proj_ref[...] = total[10:11]


def call_kernel(kernel, outputs, scratch, operands, places, flops, limit, out_places=None, aliases={}):
    out_places = out_places or "v" * len(outputs)
    spaces = {
        "v": pl.BlockSpec(memory_space=pltpu.VMEM),
        "s": pl.BlockSpec(memory_space=pltpu.SMEM),
        "h": pl.BlockSpec(memory_space=pl.ANY),
        "o": pl.BlockSpec(memory_space=pltpu.VMEM),
        "a": pl.BlockSpec(memory_space=pl.ANY),
    }
    moved = sum(array.size * array.dtype.itemsize for array in operands)
    held = {"v": pltpu.VMEM, "h": pltpu.HBM, "o": jax.ShapeDtypeStruct}
    operands = [
        pltpu.with_memory_space_constraint(array, pltpu.HBM) if place == "h" else array
        for array, place in zip(operands, places)
    ]
    return pl.pallas_call(
        kernel,
        out_shape=[held[place](*output) for output, place in zip(outputs, out_places)],
        in_specs=[spaces[place] for place in places],
        out_specs=[spaces[place] for place in out_places],
        scratch_shapes=scratch,
        input_output_aliases=aliases,
        compiler_params=pltpu.CompilerParams(vmem_limit_bytes=limit * 2**20),
        cost_estimate=pl.CostEstimate(flops=flops, bytes_accessed=moved, transcendentals=0),
    )(*operands)


def send_height(block, step):
    size = lax.axis_size("height")
    return lax.ppermute(block, "height", [(i, i ^ step) for i in range(size)])


def send_chips(block):
    return [send_height(block, step) for step in range(2, lax.axis_size("height"), 2)]


def with_cores(blocks):
    return [piece for block in blocks for piece in (block, send_height(block, 1))]


def trade_canvas(pieces):
    size = lax.axis_size("canvas")
    return [pieces[0]] + [
        lax.ppermute(piece, "canvas", [(i, i ^ step) for i in range(size)])
        for step, piece in enumerate(pieces)
        if step
    ]


def whole_canvas(
    features,
    tile_ids,
    norm_gains,
    norm_shifts,
    conv_weights,
    conv_biases,
    qkv_weight,
    qv_bias,
    proj_weight,
    proj_bias,
    cotangent,
):
    height_size = lax.axis_size("height")
    canvas_size = lax.axis_size("canvas")
    local_rows, cols, channels = features.shape[1:]
    all_rows = tile_ids.shape[1]
    pixels = all_rows * cols
    own_pixels = local_rows * cols
    out_share = channels // height_size
    ci_share = channels // canvas_size
    row_share = channels // 2 // canvas_size
    low, wide = jnp.bfloat16, jnp.float32

    own_features = features.reshape(own_pixels, channels)
    own_grad = cotangent.reshape(own_pixels, channels)
    held_features = [own_features] + send_chips(own_features)
    pieces = with_cores(held_features)
    own_grad, *pieces[::2] = lax.optimization_barrier((own_grad, *held_features))
    held_grads = [own_grad] + send_chips(own_grad)

    plane = ((pixels, channels), low)
    plane_wide = ((pixels, channels), wide)
    sums_shape = ((16, channels), wide)
    part_shapes = [((9 * out_share, ci_share), low)] * canvas_size
    mixed_shapes = [((row_share, 4 * channels), low)] * canvas_size
    taps = pltpu.VMEM((pixels + 2 * cols, 3 * channels), low)
    held_wide = pltpu.VMEM((pixels, channels), wide)
    flipped = pltpu.VMEM((channels, pixels), low)
    half_flipped = pltpu.VMEM((channels // 2, pixels), low)
    half_mixed = pltpu.VMEM((channels // 2, 4 * channels), low)
    half_qkv = pltpu.VMEM((channels // 2, 3 * channels), wide)
    half_proj = pltpu.VMEM((channels // 2, channels), wide)
    narrow = pltpu.VMEM((pixels + 2 * cols, 3 * NARROW), wide)
    columns = pltpu.VMEM((pixels, 5 * NARROW), low)
    part_held = pltpu.VMEM((5 * NARROW, channels), low)
    sem = pltpu.SemaphoreType.DMA
    conv_flops = 2 * 9 * pixels * channels * channels
    dot_flops = 2 * pixels * channels * channels
    score_flops = 2 * pixels * pixels * channels
    scale = channels ** (-0.5)

    (
        all_features,
        act_one,
        middle,
        act_two,
        residual,
        table,
        mask,
        id_rows,
        id_cols,
        turned,
        held_qkv,
        held_proj,
    ) = call_kernel(
        functools.partial(conv_kernel, cols=cols, count=height_size),
        [
            plane,
            plane,
            plane_wide,
            plane,
            plane_wide,
            ((16, channels), wide),
            ((2, pixels, LANES), wide),
            ((pixels, LANES), jnp.int32),
            ((8, pixels), jnp.int32),
            ((2, 3, channels, 3 * channels), low),
            (qkv_weight.shape, low),
            (proj_weight.shape, low),
        ],
        [
            pltpu.SMEM(tile_ids.shape, jnp.int32),
            pltpu.VMEM(norm_gains.shape, wide),
            pltpu.VMEM(norm_shifts.shape, wide),
            pltpu.VMEM(conv_biases.shape, wide),
            pltpu.VMEM(conv_weights.shape, low),
            taps,
            sem((26,)),
            sem((height_size,)),
        ],
        [
            *pieces,
            tile_ids,
            norm_gains,
            norm_shifts,
            conv_biases,
            conv_weights,
            qkv_weight,
            proj_weight,
        ],
        "h" + "a" * (height_size - 1) + "h" * 7,
        2 * conv_flops,
        24,
    )
    residual, *held_grads = lax.optimization_barrier((residual, *held_grads))
    grad_pieces = with_cores(held_grads)
    normed, query, key, value, soft, out_flip, output = call_kernel(
        functools.partial(score_kernel, score_scale=scale),
        [
            plane,
            plane,
            plane,
            plane,
            ((pixels, pixels), low),
            ((channels, pixels), low),
            ((own_pixels, channels), low),
        ],
        [
            pltpu.VMEM(qv_bias.shape, wide),
            pltpu.VMEM((1, channels), wide),
            flipped,
            sem((2,)),
        ],
        [
            qv_bias,
            proj_bias.reshape(1, channels),
            held_qkv,
            held_proj,
            residual,
            table,
            id_rows,
            id_cols,
        ],
        "hhvvvvvv",
        3 * dot_flops + 2 * score_flops,
        16,
        "v" * 6 + "o",
    )
    normed, *grad_pieces = lax.optimization_barrier((normed, *grad_pieces))
    all_grad, packed, sums, *mixed = call_kernel(
        functools.partial(attention_kernel, score_scale=scale, count=height_size),
        [plane, ((pixels, 3 * channels), low), sums_shape, *mixed_shapes],
        [
            half_mixed,
            flipped,
            held_wide,
            held_wide,
            half_flipped,
            sem((height_size,)),
        ],
        [held_proj, normed, query, key, value, soft, out_flip, *grad_pieces],
        "vvvvvvvh" + "a" * (height_size - 1),
        3 * dot_flops + 4 * score_flops,
        20,
    )
    mixed = trade_canvas(mixed)
    residual_grad, grad_two, sums, *parts_two = call_kernel(
        functools.partial(third_kernel, cols=cols),
        [plane_wide, plane, sums_shape, *part_shapes],
        [
            held_wide,
            narrow,
            columns,
            part_held,
        ],
        [held_qkv, all_grad, packed, residual, table, act_two, mask, sums],
        "vvvvvvvv",
        3 * dot_flops + conv_flops // height_size,
        16,
    )
    (act_two_grad,) = call_kernel(
        functools.partial(turn_kernel, cols=cols),
        [plane_wide],
        [taps],
        [grad_two, mask, turned],
        "vvv",
        conv_flops,
        16,
    )
    act_two_grad, *mixed = lax.optimization_barrier((act_two_grad, *mixed))
    joint_shape = (row_share * 4 * channels // LANES + 9 * out_share, LANES)
    joints = call_kernel(
        blend_kernel,
        [(joint_shape, low)] * canvas_size,
        [],
        mixed + parts_two,
        "v" * 2 * canvas_size,
        0,
        12,
    )
    joints = trade_canvas(joints)
    grad_one, sums, parts_one = call_kernel(
        functools.partial(second_kernel, cols=cols),
        [plane, sums_shape, ((canvas_size, *part_shapes[0][0]), low)],
        [held_wide, narrow, columns, part_held],
        [act_two_grad, middle, table, act_one, mask, sums],
        "vvvvvv",
        conv_flops // height_size,
        16,
    )
    parts_one = lax.all_to_all(parts_one, "canvas", 0, 0)
    input_grad, sums = call_kernel(
        functools.partial(first_kernel, cols=cols),
        [((own_pixels, channels), low), sums_shape],
        [taps, held_wide],
        [grad_one, all_features, residual_grad, table, mask, sums, turned],
        "vvvvvvv",
        conv_flops,
        16,
        "ov",
    )
    sums, *joints = lax.optimization_barrier((sums, *joints))
    qkv_grad, proj_grad, mixed_half = call_kernel(
        place_kernel,
        [(qkv_weight.shape, wide), (proj_weight.shape, wide), ((channels // 2, 4 * channels), low)],
        [half_qkv, half_proj, sem((2,))],
        joints,
        "v" * canvas_size,
        0,
        12,
        "hhv",
    )
    mixed_other = lax.ppermute(mixed_half, "height", [(i, i ^ 1) for i in range(height_size)])
    all_sums = trade_canvas([sums] * canvas_size)
    qkv_grad, proj_grad, conv_grad = call_kernel(
        join_kernel,
        [
            (qkv_weight.shape, wide),
            (proj_weight.shape, wide),
            ((2, 3, 3, out_share, ci_share), wide),
        ],
        [half_qkv, half_proj, sem((2,))],
        [qkv_grad, proj_grad, mixed_other, parts_one, *joints],
        "hhvv" + "v" * canvas_size,
        0,
        12,
        "hho",
        {0: 0, 1: 1},
    )
    vector_shapes = [norm_gains.shape, norm_shifts.shape, conv_biases.shape, qv_bias.shape]
    gains_grad, shifts_grad, biases_grad, qv_grad, proj_bias_grad = call_kernel(
        sums_kernel,
        [(shape, wide) for shape in vector_shapes + [(1, channels)]],
        [],
        all_sums,
        "v" * canvas_size,
        0,
        16,
        "ooooo",
    )
    own_shape = (1, local_rows, cols, channels)
    return (
        output.reshape(own_shape),
        input_grad.reshape(own_shape),
        gains_grad,
        shifts_grad,
        jnp.swapaxes(conv_grad, 3, 4),
        biases_grad,
        qkv_grad,
        qv_grad,
        proj_grad,
        proj_bias_grad.reshape(channels),
    )


def on_device(*arrays):
    features, tile_ids = arrays[0], arrays[1]
    local_rows, cols, channels = features.shape[1:]
    pixels = tile_ids.shape[1] * cols
    height_size, canvas_size = lax.axis_size("height"), lax.axis_size("canvas")
    powers = all(size & (size - 1) == 0 for size in (height_size, canvas_size, cols))
    fits = (
        powers
        and height_size > 1
        and channels == LANES * canvas_size
        and pixels <= MOST_PIXELS
        and pixels % CONV_ROWS == 0
        and (local_rows * cols) % LANES == 0
        and CHUNK % cols == 0
        and cols % 16 == 0
        and channels % (LANES * canvas_size) == 0
        and 2 * channels == NARROW * height_size
    )
    return whole_canvas(*arrays) if fits else split_canvas(*arrays)


def solution(mesh):
    in_specs = (
        P("canvas", "height", None, None),
        P("canvas", None),
        P(),
        P(),
        P(),
        P(),
        P(),
        P(),
        P(),
        P(),
        P("canvas", "height", None, None),
    )
    out_specs = (
        P("canvas", "height", None, None),
        P("canvas", "height", None, None),
        P(),
        P(),
        P(None, None, None, "canvas", "height"),
        P(),
        P(),
        P(),
        P(),
        P(),
    )
    return jax.shard_map(
        on_device, mesh=mesh, in_specs=in_specs, out_specs=out_specs, check_vma=False
    )
```

```python
import functools

import jax
import jax.numpy as jnp
from jax import lax
from jax.experimental import pallas as pl
from jax.experimental.pallas import tpu as pltpu
from jax.sharding import PartitionSpec as P

GROUPS = 32


epsilon = 1e-06
masked_score = -1e30
MOST_PIXELS = 1024
LANES = 128
NARROW = 128
CHUNK = 128
CONV_ROWS = 1024
FILL_ROWS = 256
QUERY_ROWS = 512


def extended(block, sides, width):
    for axis, dim in sides:
        count = lax.axis_size(axis)
        forward = [(i, i + 1) for i in range(count - 1)]
        backward = [(target, source) for source, target in forward]
        low = lax.ppermute(
            lax.slice_in_dim(block, block.shape[dim] - width, None, axis=dim), axis, forward
        )
        high = lax.ppermute(lax.slice_in_dim(block, 0, width, axis=dim), axis, backward)
        block = jnp.concatenate([low, block, high], axis=dim)
    return block


def group_total(vector):
    return vector.reshape(GROUPS, -1).sum(axis=1)


def spread_groups(vector, channels):
    return jnp.repeat(vector, channels // GROUPS)


def norm_forward(values, gain, shift, members):
    channels = values.shape[1]
    totals = lax.psum(group_total(jnp.sum(values, axis=0)), "height")
    centered = values - spread_groups(totals / members, channels)
    squares = lax.psum(group_total(jnp.sum(centered * centered, axis=0)), "height")
    inverse = spread_groups(lax.rsqrt(squares / members + epsilon), channels)
    normed = centered * inverse
    return (normed, inverse, normed * gain + shift)


def norm_backward(grad_in, normed, inverse, gain, members):
    channels = grad_in.shape[1]
    scaled = grad_in * gain
    both_sums = lax.psum(
        (group_total(jnp.sum(scaled, axis=0)), group_total(jnp.sum(scaled * normed, axis=0))),
        "height",
    )
    mean_grad = spread_groups(both_sums[0] / members, channels)
    mean_cross = spread_groups(both_sums[1] / members, channels)
    result = inverse * (scaled - mean_grad - normed * mean_cross)
    return (result, jnp.sum(grad_in * normed, axis=0), jnp.sum(grad_in, axis=0))


def swish(values):
    return values * jax.nn.sigmoid(values)


def swish_slope(values):
    sigmoid_part = jax.nn.sigmoid(values)
    return sigmoid_part * (1.0 + values * (1.0 - sigmoid_part))


def tap_columns(padded, row_mask, local_rows, canvas_cols):
    pieces = []
    for row_tap in range(3):
        rows_taken = padded[row_tap : row_tap + local_rows] * row_mask[:, row_tap, None, None]
        for col_tap in range(3):
            pieces.append(rows_taken[:, col_tap : col_tap + canvas_cols])
    stacked = jnp.concatenate(pieces, axis=2)
    return stacked.reshape(local_rows * canvas_cols, stacked.shape[2])


def conv_forward(acts, row_mask, weight, bias):
    local_rows, canvas_cols, channels = acts.shape
    rimmed = extended(acts, (("height", 0),), 1)
    padded = jnp.pad(rimmed, ((0, 0), (1, 1), (0, 0)))
    gathered = tap_columns(padded, row_mask, local_rows, canvas_cols)
    result = (
        jnp.dot(
            gathered, weight.reshape(9 * channels, channels), preferred_element_type=jnp.float32
        )
        + bias
    )
    return (result, gathered)


def conv_backward(grad_low, row_mask, weight, gathered):
    local_rows, canvas_cols, channels = grad_low.shape
    flat_grad = grad_low.reshape(local_rows * canvas_cols, channels)
    weight_grad = lax.dot_general(
        gathered, flat_grad, (((0,), (0,)), ((), ())), preferred_element_type=jnp.float32
    )
    rimmed = extended(grad_low, (("height", 0),), 1)
    padded = jnp.pad(rimmed, ((0, 0), (1, 1), (0, 0)))
    grad_taps = tap_columns(padded, row_mask, local_rows, canvas_cols)
    flipped = jnp.transpose(weight[::-1, ::-1], (0, 1, 3, 2)).reshape(9 * channels, channels)
    input_part = jnp.dot(grad_taps, flipped, preferred_element_type=jnp.float32)
    return (
        input_part,
        weight_grad.reshape(3, 3, channels, channels),
        jnp.sum(flat_grad.astype(jnp.float32), axis=0),
    )


def take_rows(array, offset, count):
    return lax.dynamic_slice_in_dim(array, offset, count)


def score_grads(
    queries, out_grad, log_total, row_dots, query_ids, key_rows, value_rows, key_ids, score_scale
):
    scores = (
        lax.dot_general(
            queries, key_rows, (((1,), (1,)), ((), ())), preferred_element_type=jnp.float32
        )
        * score_scale
    )
    same_tile = query_ids[:, None] == key_ids[None, :]
    softmax_block = jnp.exp(jnp.where(same_tile, scores - log_total[:, None], masked_score))
    weight_grad = lax.dot_general(
        out_grad, value_rows, (((1,), (1,)), ((), ())), preferred_element_type=jnp.float32
    )
    score_grad = (softmax_block * (weight_grad - row_dots[:, None])).astype(jnp.bfloat16)
    return (softmax_block.astype(jnp.bfloat16), score_grad)


def split_canvas(
    features,
    tile_ids,
    norm_gains,
    norm_shifts,
    conv_weights,
    conv_biases,
    qkv_weight,
    qv_bias,
    proj_weight,
    proj_bias,
    cotangent,
):
    height_size = lax.axis_size("height")
    local_rows = features.shape[1]
    canvas_cols = features.shape[2]
    channels = features.shape[3]
    pixels = local_rows * canvas_cols
    row_ids = tile_ids[0]
    all_rows = row_ids.shape[0]
    members = float(all_rows * canvas_cols * (channels // GROUPS))
    score_scale = channels ** (-0.5)
    first_row = lax.axis_index("height") * local_rows
    edge_ids = jnp.full((1,), -1, jnp.int32)
    padded_ids = jnp.concatenate([edge_ids, row_ids, edge_ids])
    near_ids = lax.dynamic_slice_in_dim(padded_ids, first_row, local_rows + 2)
    own_rows = near_ids[1 : local_rows + 1]
    row_mask = jnp.stack(
        [near_ids[row_tap : row_tap + local_rows] == own_rows for row_tap in range(3)], axis=1
    ).astype(jnp.bfloat16)
    key_ids = jnp.repeat(row_ids, canvas_cols)
    query_ids = jnp.repeat(own_rows, canvas_cols)
    grid_shape = (local_rows, canvas_cols, channels)
    inputs = features[0].reshape(pixels, channels).astype(jnp.float32)
    normed_one, inverse_one, pre_one = norm_forward(inputs, norm_gains[0], norm_shifts[0], members)
    act_one = swish(pre_one).astype(jnp.bfloat16).reshape(grid_shape)
    middle, taps_one = conv_forward(act_one, row_mask, conv_weights[0], conv_biases[0])
    normed_two, inverse_two, pre_two = norm_forward(middle, norm_gains[1], norm_shifts[1], members)
    act_two = swish(pre_two).astype(jnp.bfloat16).reshape(grid_shape)
    branch, taps_two = conv_forward(act_two, row_mask, conv_weights[1], conv_biases[1])
    residual = inputs + branch
    normed_three, inverse_three, pre_three = norm_forward(
        residual, norm_gains[2], norm_shifts[2], members
    )
    attn_input = pre_three.astype(jnp.bfloat16)
    mixed = jnp.dot(attn_input, qkv_weight, preferred_element_type=jnp.float32)
    queries = (mixed[:, :channels] + qv_bias[0]).astype(jnp.bfloat16)
    key_rows = mixed[:, channels : 2 * channels].astype(jnp.bfloat16)
    value_rows = (mixed[:, 2 * channels :] + qv_bias[1]).astype(jnp.bfloat16)
    running_max = jnp.full((pixels,), masked_score, jnp.float32)
    key_piece = lax.all_gather(key_rows, "height", axis=0, tiled=True)
    value_piece = lax.all_gather(value_rows, "height", axis=0, tiled=True)
    scores = (
        lax.dot_general(
            queries, key_piece, (((1,), (1,)), ((), ())), preferred_element_type=jnp.float32
        )
        * score_scale
    )
    same_tile = query_ids[:, None] == key_ids[None, :]
    scores = jnp.where(same_tile, scores, masked_score)
    new_max = jnp.maximum(running_max, jnp.max(scores, axis=1))
    weights = jnp.where(same_tile, jnp.exp(scores - new_max[:, None]), 0.0)
    summed_out = jnp.dot(
        weights.astype(jnp.bfloat16), value_piece, preferred_element_type=jnp.float32
    )
    total_weight = jnp.sum(weights, axis=1)
    log_total = new_max + jnp.log(total_weight)
    attended = summed_out / total_weight[:, None]
    attended_low = attended.astype(jnp.bfloat16)
    output = (
        residual
        + jnp.dot(attended_low, proj_weight, preferred_element_type=jnp.float32)
        + proj_bias
    )
    out_grad = cotangent[0].reshape(pixels, channels)
    out_grad_full = out_grad.astype(jnp.float32)
    proj_grad = lax.dot_general(
        attended_low, out_grad, (((0,), (0,)), ((), ())), preferred_element_type=jnp.float32
    )
    proj_bias_grad = jnp.sum(out_grad_full, axis=0)
    attended_grad = lax.dot_general(
        out_grad, proj_weight, (((1,), (1,)), ((), ())), preferred_element_type=jnp.float32
    ).astype(jnp.bfloat16)
    row_dots = jnp.sum(attended_grad.astype(jnp.float32) * attended, axis=1)
    block_rows = pixels * min(height_size, 8)
    zero_block = jnp.zeros((pixels, channels), jnp.float32)
    key_all, value_all = (
        lax.all_gather(key_rows, "height", axis=0, tiled=True),
        lax.all_gather(value_rows, "height", axis=0, tiled=True),
    )
    query_all, grad_all = (
        lax.all_gather(queries, "height", axis=0, tiled=True),
        lax.all_gather(attended_grad, "height", axis=0, tiled=True),
    )
    total_all, dots_all = (
        lax.all_gather(log_total, "height", axis=0, tiled=True),
        lax.all_gather(row_dots, "height", axis=0, tiled=True),
    )

    def own_query_step(running, block_index):
        offset = block_index * block_rows
        key_part = take_rows(key_all, offset, block_rows)
        rounded, score_grad = score_grads(
            queries,
            attended_grad,
            log_total,
            row_dots,
            query_ids,
            key_part,
            take_rows(value_all, offset, block_rows),
            take_rows(key_ids, offset, block_rows),
            score_scale,
        )
        return (
            running
            + jnp.dot(score_grad, key_part, preferred_element_type=jnp.float32) * score_scale,
            None,
        )

    def own_key_step(running, block_index):
        offset = block_index * block_rows
        query_part = take_rows(query_all, offset, block_rows)
        grad_part = take_rows(grad_all, offset, block_rows)
        rounded, score_grad = score_grads(
            query_part,
            grad_part,
            take_rows(total_all, offset, block_rows),
            take_rows(dots_all, offset, block_rows),
            take_rows(key_ids, offset, block_rows),
            key_rows,
            value_rows,
            query_ids,
            score_scale,
        )
        key_part = (
            lax.dot_general(
                score_grad, query_part, (((0,), (0,)), ((), ())), preferred_element_type=jnp.float32
            )
            * score_scale
        )
        value_part = lax.dot_general(
            rounded, grad_part, (((0,), (0,)), ((), ())), preferred_element_type=jnp.float32
        )
        return ((running[0] + key_part, running[1] + value_part), None)

    block_count = key_all.shape[0] // block_rows
    query_grad, unused_one = lax.scan(own_query_step, zero_block, jnp.arange(block_count))
    (key_grad, value_grad), unused_two = lax.scan(
        own_key_step, (zero_block, zero_block), jnp.arange(block_count)
    )
    query_low = query_grad.astype(jnp.bfloat16)
    key_low = key_grad.astype(jnp.bfloat16)
    value_low = value_grad.astype(jnp.bfloat16)
    stacked_grad = jnp.concatenate([query_low, key_low, value_low], axis=1)
    qkv_grad = lax.dot_general(
        attn_input, stacked_grad, (((0,), (0,)), ((), ())), preferred_element_type=jnp.float32
    )
    qv_grad = jnp.stack(
        [
            jnp.sum(query_low.astype(jnp.float32), axis=0),
            jnp.sum(value_low.astype(jnp.float32), axis=0),
        ]
    )
    normed_grad = lax.dot_general(
        stacked_grad, qkv_weight, (((1,), (1,)), ((), ())), preferred_element_type=jnp.float32
    )
    back_three, gain_three, shift_three = norm_backward(
        normed_grad, normed_three, inverse_three, norm_gains[2], members
    )
    residual_grad = out_grad_full + back_three
    grad_two = residual_grad.astype(jnp.bfloat16).reshape(grid_shape)
    act_two_grad, weight_two_grad, bias_two_grad = conv_backward(
        grad_two, row_mask, conv_weights[1], taps_two
    )
    middle_grad, gain_two, shift_two = norm_backward(
        act_two_grad * swish_slope(pre_two), normed_two, inverse_two, norm_gains[1], members
    )
    grad_one = middle_grad.astype(jnp.bfloat16).reshape(grid_shape)
    act_one_grad, weight_one_grad, bias_one_grad = conv_backward(
        grad_one, row_mask, conv_weights[0], taps_one
    )
    input_back, gain_one, shift_one = norm_backward(
        act_one_grad * swish_slope(pre_one), normed_one, inverse_one, norm_gains[0], members
    )
    input_grad = residual_grad + input_back
    conv_grad = jnp.stack([weight_one_grad, weight_two_grad])
    conv_part = lax.psum_scatter(conv_grad, "height", scatter_dimension=4, tiled=True)
    conv_part = lax.psum_scatter(
        conv_part.astype(jnp.bfloat16), "canvas", scatter_dimension=3, tiled=True
    ).astype(jnp.float32)
    summed = lax.psum(
        (
            jnp.stack([gain_one, gain_two, gain_three]),
            jnp.stack([shift_one, shift_two, shift_three]),
            jnp.stack([bias_one_grad, bias_two_grad]),
            qkv_grad,
            qv_grad,
            proj_grad,
            proj_bias_grad,
        ),
        ("canvas", "height"),
    )
    return (
        output.astype(jnp.bfloat16).reshape((1,) + grid_shape),
        input_grad.astype(jnp.bfloat16).reshape((1,) + grid_shape),
        summed[0],
        summed[1],
        conv_part,
        summed[2],
        summed[3],
        summed[4],
        summed[5],
        summed[6],
    )


def fold(block):
    rows, width = block.shape
    return jnp.sum(block.reshape(rows // 8, 8, width), axis=0)


def group_lanes(block, group):
    lane = lax.broadcasted_iota(jnp.int32, block.shape, 1)
    width = block.shape[1]
    step = 1
    while step < group:
        above = pltpu.roll(block, step, 1)
        below = pltpu.roll(block, width - step, 1)
        block = block + jnp.where((lane & step) != 0, above, below)
        step *= 2
    return block


def group_mean(partial, members):
    spread = group_lanes(partial, partial.shape[1] // GROUPS)
    return jnp.sum(spread, axis=0, keepdims=True) * (1.0 / members)


def widen(block, width):
    return jnp.concatenate([block] * (width // block.shape[1]), axis=1)


def each_chunk(pixels, body, carry):
    def step(index, carry):
        return body(pl.ds(pl.multiple_of(index * CHUNK, CHUNK), CHUNK), carry)

    return lax.fori_loop(0, pixels // CHUNK, step, carry)


def aligned(start, step):
    return start if isinstance(start, int) else pl.multiple_of(start, step)


def fold_about(block, center):
    rows, width = block.shape
    offset = block.reshape(rows // 8, 8, width) - center[None]
    return jnp.sum(offset, axis=0), jnp.sum(offset * offset, axis=0)


def finish_stats(center, sums, squares, pixels):
    width = center.shape[1] // GROUPS
    share = pixels / 8.0
    means = center + sums * (1.0 / share)
    spread = squares - sums * sums * (1.0 / share)
    mean = group_mean(means, 8.0 * width)
    offset = means - mean
    variance = group_mean(spread + share * offset * offset, float(pixels * width))
    return mean, lax.rsqrt(variance + epsilon)


def norm_stats(read, pixels, channels):
    center = read(pl.ds(0, 8))
    zeros = jnp.zeros((8, channels), jnp.float32)

    def step(rows, carry):
        sums, squares = fold_about(read(rows), center)
        return carry[0] + sums, carry[1] + squares

    return finish_stats(center, *each_chunk(pixels, step, (zeros, zeros)), pixels)


class RunningStats:
    def __init__(self):
        self.center = None

    def add(self, block):
        if self.center is None:
            self.center = block[0:8]
            self.sums, self.squares = fold_about(block, self.center)
        else:
            sums, squares = fold_about(block, self.center)
            self.sums, self.squares = self.sums + sums, self.squares + squares

    def finish(self, pixels):
        return finish_stats(self.center, self.sums, self.squares, pixels)


def put_taps(taps_ref, block, rows, cols):
    count, channels = block.shape
    place = lax.broadcasted_iota(jnp.int32, block.shape, 0) & (cols - 1)
    left = jnp.where(place == 0, 0.0, pltpu.roll(block, 1, 0))
    right = jnp.where(place == cols - 1, 0.0, pltpu.roll(block, count - 1, 0))
    inner = pl.ds(aligned(rows.start + cols, cols), count)
    taps_ref[inner, 0:channels] = left.astype(jnp.bfloat16)
    taps_ref[inner, channels : 2 * channels] = block.astype(jnp.bfloat16)
    taps_ref[inner, 2 * channels :] = right.astype(jnp.bfloat16)


def clear_edges(taps_ref, cols):
    edge = jnp.zeros((cols, taps_ref.shape[1]), taps_ref.dtype)
    taps_ref[0:cols, :] = edge
    taps_ref[taps_ref.shape[0] - cols :, :] = edge


def run_conv(taps_ref, product, mask_ref, total_ref, fill, first, last, cols):
    pixels, channels = total_ref.shape
    for start in range(0, pixels, FILL_ROWS):
        for inner in range(start, start + FILL_ROWS, CHUNK):
            fill(pl.ds(inner, CHUNK))
        rows = pl.ds(start, FILL_ROWS)
        total_ref[rows, :] = first(rows, product(taps_ref, pl.ds(start + cols, FILL_ROWS), 1))
    block = min(CONV_ROWS, pixels)
    for row_tap in (0, 2):
        for start in range(0, pixels, block):
            rows = pl.ds(start, block)
            part = product(taps_ref, pl.ds(start + row_tap * cols, block), row_tap)
            mask = widen(mask_ref[row_tap // 2, rows, :], channels)
            value = total_ref[rows, :] + mask * part
            total_ref[rows, :] = value if row_tap == 0 else last(rows, value)


def product_forward(weight_ref):
    channels = weight_ref.shape[-1]

    def product(taps_ref, shifted, row_tap):
        return jnp.dot(
            taps_ref[shifted, :],
            weight_ref[row_tap].reshape(3 * channels, channels),
            preferred_element_type=jnp.float32,
        )

    return product


def product_backward(weight_ref):
    def product(taps_ref, shifted, row_tap):
        return lax.dot_general(
            taps_ref[shifted, :],
            weight_ref[row_tap],
            (((1,), (1,)), ((), ())),
            preferred_element_type=jnp.float32,
        )

    return product


def smooth(values):
    part = 0.5 * jnp.tanh(0.5 * values) + 0.5
    return values * part, part


def activation(read, mean, inverse, gain, shift, act_ref, taps_ref, cols):
    scale = inverse * gain

    def fill(rows):
        act = smooth((read(rows) - mean) * scale + shift)[0]
        act_ref[rows, :] = act.astype(jnp.bfloat16)
        put_taps(taps_ref, act, rows, cols)

    return fill


def back_means(sums, gain, pixels):
    channels = gain.shape[1]
    members = float(pixels * (channels // GROUPS))
    return group_mean(sums[0] * gain, members), group_mean(sums[1] * gain, members)


def column_total(partial):
    return jnp.sum(partial, axis=0, keepdims=True)


def weight_part(act_ref, grad_ref, mask_ref, narrow_ref, columns_ref, part_ref, cols):
    pixels, channels = act_ref.shape
    height = lax.axis_index("height")
    share = NARROW // 2
    block = pl.ds(pl.multiple_of((height // 2) * NARROW, NARROW), NARROW)
    parity = height % 2
    edge = jnp.zeros((cols, 3 * NARROW), jnp.float32)
    narrow_ref[0:cols, :] = edge
    narrow_ref[cols + pixels :, :] = edge

    def spread(rows, carry):
        own = grad_ref[rows, block].astype(jnp.float32)
        half = lax.broadcasted_iota(jnp.int32, own.shape, 1) // share
        turned = pltpu.roll(own, share, 1)
        both = jnp.where(half == parity, own, turned)
        place = lax.broadcasted_iota(jnp.int32, own.shape, 0) & (cols - 1)
        left = jnp.where(place == 0, 0.0, pltpu.roll(both, 1, 0))
        right = jnp.where(place == cols - 1, 0.0, pltpu.roll(both, CHUNK - 1, 0))
        inner = pl.ds(pl.multiple_of(rows.start + cols, cols), CHUNK)
        narrow_ref[inner, 0:NARROW] = left
        narrow_ref[inner, NARROW : 2 * NARROW] = both
        narrow_ref[inner, 2 * NARROW :] = right
        return carry

    each_chunk(pixels, spread, 0)

    def gather(rows, carry):
        taps = []
        for row_tap in range(3):
            for col_tap in range(3):
                row_back, col_back = 2 - row_tap, 2 - col_tap
                shifted = pl.ds(pl.multiple_of(rows.start + row_back * cols, cols), CHUNK)
                block = narrow_ref[shifted, col_back * NARROW : (col_back + 1) * NARROW]
                if row_back != 1:
                    block = block * mask_ref[row_back // 2, rows, :]
                taps.append(block)
        lower = lax.broadcasted_iota(jnp.int32, taps[0].shape, 1) < share
        for pair in range(5):
            second = taps[min(2 * pair + 1, 8)]
            columns_ref[rows, pair * NARROW : (pair + 1) * NARROW] = jnp.where(
                lower, taps[2 * pair], second
            ).astype(jnp.bfloat16)
        return carry

    each_chunk(pixels, gather, 0)
    part_ref[...] = lax.dot_general(
        columns_ref[...],
        act_ref[...],
        (((0,), (0,)), ((), ())),
        preferred_element_type=jnp.float32,
    ).astype(jnp.bfloat16)


def conv_back(grad_ref, weights_ref, mask_ref, taps_ref, total_ref, read, table_ref, which, cols):
    clear_edges(taps_ref, cols)
    mean, inverse, gain, shift = norm_rows(table_ref, which)
    sums = []

    def fill(rows):
        put_taps(taps_ref, grad_ref[rows, :].astype(jnp.float32), rows, cols)

    def slope(rows, value):
        normed = (read(rows) - mean) * inverse
        pre = normed * gain + shift
        part = smooth(pre)[1]
        grad = value * (part * (1.0 + pre * (1.0 - part)))
        sums.append((fold(grad), fold(grad * normed)))
        return grad

    run_conv(
        taps_ref,
        product_backward(weights_ref),
        mask_ref,
        total_ref,
        fill,
        lambda rows, part: part,
        slope,
        cols,
    )
    return sum(pair[0] for pair in sums), sum(pair[1] for pair in sums)


def norm_back(total_ref, sums, read, table_ref, which):
    mean, inverse, gain, shift = norm_rows(table_ref, which)
    mean_grad, mean_cross = back_means(sums, gain, total_ref.shape[0])

    def back(rows):
        normed = (read(rows) - mean) * inverse
        return inverse * (total_ref[rows, :] * gain - mean_grad - normed * mean_cross)

    return back


def turn_kernel(
    grad_ref, mask_ref, weights_ref, middle_ref, table_ref, total_ref, sums_ref, taps_ref, *, cols
):
    sums_ref[0:8, :], sums_ref[8:16, :] = conv_back(
        grad_ref,
        weights_ref.at[1],
        mask_ref,
        taps_ref,
        total_ref,
        lambda rows: middle_ref[rows, :],
        table_ref,
        1,
        cols,
    )


def norm_rows(table_ref, which):
    picks = (2 * which, 2 * which + 1, 6 + which, 9 + which)
    return tuple(table_ref[pick : pick + 1, :] for pick in picks)


def build_masks(ids_ref, mask_ref, id_rows_ref, id_cols_ref, cols):
    rows = ids_ref.shape[1]
    for row in range(rows):
        here = ids_ref[0, row]
        place = slice(row * cols, (row + 1) * cols)
        id_rows_ref[place, :] = jnp.full((cols, LANES), here, jnp.int32)
        for side, other in ((0, row - 1), (1, row + 1)):
            same = jnp.float32(0.0)
            if 0 <= other < rows:
                same = jnp.where(ids_ref[0, other] == here, 1.0, 0.0).astype(jnp.float32)
            mask_ref[side, place, :] = jnp.full((cols, LANES), same, jnp.float32)
    lane = lax.broadcasted_iota(jnp.int32, (8, LANES), 1)
    each = LANES // cols
    for block in range(rows // each):
        ids = jnp.full((8, LANES), ids_ref[0, block * each], jnp.int32)
        for step in range(1, each):
            ids = jnp.where(lane >= step * cols, ids_ref[0, block * each + step], ids)
        id_cols_ref[:, block * LANES : (block + 1) * LANES] = ids


def place_pieces(pieces, whole_ref, sems):
    own_pixels = whole_ref.shape[0] // len(pieces)
    height = lax.axis_index("height")
    copies = []
    for place, piece in enumerate(pieces):
        start = pl.multiple_of((height ^ place) * own_pixels, own_pixels)
        rows = pl.ds(start, own_pixels)
        copies.append(pltpu.make_async_copy(piece, whole_ref.at[rows, :], sems.at[place]))
    return copies


def conv_kernel(*refs, cols, count):
    pieces, refs = refs[:count], refs[count:]
    (
        ids_hbm,
        gains_hbm,
        shifts_hbm,
        biases_hbm,
        weights_hbm,
        qkv_hbm,
        proj_hbm,
        features_ref,
        act_one_ref,
        middle_ref,
        act_two_ref,
        residual_ref,
        table_ref,
        mask_ref,
        id_rows_ref,
        id_cols_ref,
        turned_ref,
        qkv_ref,
        proj_ref,
        ids_ref,
        gains_ref,
        shifts_ref,
        biases_ref,
        weights_ref,
        taps_ref,
        sems,
        piece_sems,
    ) = refs
    pixels, channels = features_ref.shape
    wide = jnp.float32
    turned = [
        (
            weights_hbm.at[which, 2 - row_tap, 2 - col_tap],
            turned_ref.at[which, row_tap, :, col_tap * channels : (col_tap + 1) * channels],
        )
        for which in (1, 0)
        for row_tap in range(3)
        for col_tap in range(3)
    ]
    arrivals = place_pieces(pieces, features_ref, piece_sems)
    moves = [
        (ids_hbm, ids_ref),
        (gains_hbm, gains_ref),
        (shifts_hbm, shifts_ref),
        (weights_hbm.at[0], weights_ref.at[0]),
        (biases_hbm, biases_ref),
        (weights_hbm.at[1], weights_ref.at[1]),
        (qkv_hbm, qkv_ref),
        (proj_hbm, proj_ref),
    ] + turned
    copies = [
        pltpu.make_async_copy(source, target, sems.at[index])
        for index, (source, target) in enumerate(moves)
    ]
    for copy in copies[:1] + arrivals + copies[1:6]:
        copy.start()
    clear_edges(taps_ref, cols)
    copies[0].wait()
    build_masks(ids_ref, mask_ref, id_rows_ref, id_cols_ref, cols)
    for copy in arrivals:
        copy.wait()

    def read_input(rows):
        return features_ref[rows, :].astype(wide)

    def read_middle(rows):
        return middle_ref[rows, :]

    table_ref[0:1, :], table_ref[1:2, :] = norm_stats(read_input, pixels, channels)
    copies[1].wait()
    copies[2].wait()
    table_ref[6:9, :] = gains_ref[...]
    table_ref[9:12, :] = shifts_ref[...]
    for copy in copies[6:]:
        copy.start()
    copies[3].wait()
    copies[4].wait()
    seen = RunningStats()

    def keep(rows, value):
        seen.add(value)
        return value

    run_conv(
        taps_ref,
        product_forward(weights_ref.at[0]),
        mask_ref,
        middle_ref,
        activation(read_input, *norm_rows(table_ref, 0), act_one_ref, taps_ref, cols),
        lambda rows, part: part + biases_ref[0:1, :],
        keep,
        cols,
    )
    table_ref[2:3, :], table_ref[3:4, :] = seen.finish(pixels)
    copies[5].wait()
    seen = RunningStats()
    run_conv(
        taps_ref,
        product_forward(weights_ref.at[1]),
        mask_ref,
        residual_ref,
        activation(read_middle, *norm_rows(table_ref, 1), act_two_ref, taps_ref, cols),
        lambda rows, part: part + (read_input(rows) + biases_ref[1:2, :]),
        keep,
        cols,
    )
    table_ref[4:5, :], table_ref[5:6, :] = seen.finish(pixels)
    for copy in copies[6:]:
        copy.wait()


def score_kernel(
    qv_bias_hbm,
    proj_bias_hbm,
    qkv_ref,
    proj_ref,
    residual_ref,
    table_ref,
    id_rows_ref,
    id_cols_ref,
    normed_ref,
    query_ref,
    key_ref,
    value_ref,
    soft_ref,
    out_flip_ref,
    output_ref,
    qv_bias_ref,
    proj_bias_ref,
    value_flip_ref,
    sems,
    *,
    score_scale,
):
    pixels, channels = residual_ref.shape
    own_pixels = output_ref.shape[0]
    wide = jnp.float32
    exponent = score_scale * 1.4426950408889634
    moves = [(qv_bias_hbm, qv_bias_ref), (proj_bias_hbm, proj_bias_ref)]
    copies = [
        pltpu.make_async_copy(source, target, sems.at[index])
        for index, (source, target) in enumerate(moves)
    ]
    for copy in copies:
        copy.start()
    mean, inverse, gain, shift = norm_rows(table_ref, 2)
    scale = inverse * gain
    for copy in copies:
        copy.wait()
    block = min(QUERY_ROWS, pixels)

    def project(index, carry):
        rows = pl.ds(pl.multiple_of(index * block, block), block)
        normed = ((residual_ref[rows, :] - mean) * scale + shift).astype(jnp.bfloat16)
        normed_ref[rows, :] = normed
        query_ref[rows, :] = (
            jnp.dot(normed, qkv_ref[:, 0:channels], preferred_element_type=wide)
            + qv_bias_ref[0:1, :]
        ).astype(jnp.bfloat16)
        key_ref[rows, :] = jnp.dot(
            normed, qkv_ref[:, channels : 2 * channels], preferred_element_type=wide
        ).astype(jnp.bfloat16)
        values = (
            jnp.dot(normed, qkv_ref[:, 2 * channels :], preferred_element_type=wide)
            + qv_bias_ref[1:2, :]
        ).astype(jnp.bfloat16)
        value_ref[rows, :] = values
        value_flip_ref[:, rows] = values.T
        return carry

    lax.fori_loop(0, pixels // block, project, 0)

    def attend(index, carry):
        rows = pl.ds(pl.multiple_of(index * block, block), block)
        scores = lax.dot_general(
            key_ref[...], query_ref[rows, :], (((1,), (1,)), ((), ())), preferred_element_type=wide
        )
        same = widen(id_rows_ref[...], block) == id_cols_ref[0:1, rows]
        scores = jnp.where(same, scores, masked_score)
        scores = jnp.exp2((scores - jnp.max(scores, axis=0, keepdims=True)) * exponent)
        weights = scores * (1.0 / jnp.sum(scores, axis=0, keepdims=True))
        rounded = weights.astype(jnp.bfloat16)
        soft_ref[:, rows] = rounded
        out_flip_ref[:, rows] = jnp.dot(
            value_flip_ref[...], rounded, preferred_element_type=wide
        ).astype(jnp.bfloat16)
        return carry

    lax.fori_loop(0, pixels // block, attend, 0)
    height = lax.axis_index("height")
    own = pl.ds(pl.multiple_of(height * own_pixels, own_pixels), own_pixels)
    output_ref[...] = (
        residual_ref[own, :]
        + lax.dot_general(
            out_flip_ref[:, own],
            proj_ref[...],
            (((0,), (0,)), ((), ())),
            preferred_element_type=wide,
        )
        + proj_bias_ref[...]
    ).astype(jnp.bfloat16)


def own_quarter():
    height = lax.axis_index("height")
    return (height & 1) * 2 + ((height >> 1) & 1)


def send_order(source_ref, targets, axis, share):
    me = lax.axis_index("canvas")
    for step, target in enumerate(targets):
        place = pl.ds(pl.multiple_of((me ^ step) * share, share), share)
        target[...] = source_ref[place, :] if axis == 0 else source_ref[:, place]


def attention_kernel(
    proj_ref,
    normed_ref,
    query_ref,
    key_ref,
    value_ref,
    soft_ref,
    out_flip_ref,
    *refs,
    score_scale,
    count,
):
    pieces, (grad_ref, packed_ref, sums_ref), refs = (
        refs[:count],
        refs[count : count + 3],
        refs[count + 3 :],
    )
    *mixed_refs, mixed_ref, key_flip_ref, key_sum_ref, value_sum_ref, flip_ref, sems = refs
    pixels, channels = normed_ref.shape
    block = min(QUERY_ROWS, pixels)
    wide = jnp.float32
    copies = place_pieces(pieces, grad_ref, sems)
    for copy in copies:
        copy.start()
    quarter = channels // 4
    own = pl.ds(pl.multiple_of(own_quarter() * quarter, quarter), quarter)
    flip_ref[...] = normed_ref[:, own].T
    key_flip_ref[...] = key_ref[...].T
    key_sum_ref[...] = jnp.zeros(key_sum_ref.shape, wide)
    value_sum_ref[...] = jnp.zeros(value_sum_ref.shape, wide)
    for copy in copies:
        copy.wait()

    def attend(index, carry):
        rows = pl.ds(pl.multiple_of(index * block, block), block)
        back = lax.dot_general(
            grad_ref[rows, :], proj_ref[...], (((1,), (1,)), ((), ())), preferred_element_type=wide
        ).astype(jnp.bfloat16)
        rounded = soft_ref[:, rows]
        weights = rounded.astype(wide)
        weight_grad = lax.dot_general(
            value_ref[...], back, (((1,), (1,)), ((), ())), preferred_element_type=wide
        )
        value_sum_ref[...] += jnp.dot(rounded, back, preferred_element_type=wide)
        dots = jnp.sum(weights * weight_grad, axis=0, keepdims=True)
        score_grad = (weights * (weight_grad - dots)).astype(jnp.bfloat16)
        key_sum_ref[...] += jnp.dot(score_grad, query_ref[rows, :], preferred_element_type=wide)
        query_grad = jnp.dot(key_flip_ref[...], score_grad, preferred_element_type=wide)
        packed_ref[rows, 0:channels] = (query_grad * score_scale).astype(jnp.bfloat16).T
        return carry

    lax.fori_loop(0, pixels // block, attend, 0)

    def pack(rows, carry):
        packed_ref[rows, channels : 2 * channels] = (key_sum_ref[rows, :] * score_scale).astype(
            jnp.bfloat16
        )
        packed_ref[rows, 2 * channels :] = value_sum_ref[rows, :].astype(jnp.bfloat16)
        return (
            carry[0] + fold(packed_ref[rows, 0:channels].astype(wide)),
            carry[1] + fold(packed_ref[rows, 2 * channels :].astype(wide)),
            carry[2] + fold(grad_ref[rows, :].astype(wide)),
        )

    zeros = jnp.zeros((8, channels), wide)
    totals = each_chunk(pixels, pack, (zeros, zeros, zeros))
    sums_ref[...] = jnp.zeros(sums_ref.shape, wide)
    for row, total in enumerate(totals):
        sums_ref[8 + row : 9 + row, :] = column_total(total)

    mixed_ref[:, 0 : 3 * channels] = jnp.dot(
        flip_ref[...], packed_ref[...], preferred_element_type=wide
    ).astype(jnp.bfloat16)
    mixed_ref[:, 3 * channels :] = jnp.dot(
        out_flip_ref[own, :], grad_ref[...], preferred_element_type=wide
    ).astype(jnp.bfloat16)
    send_order(mixed_ref, mixed_refs, 0, quarter // len(mixed_refs))


def third_kernel(
    qkv_ref,
    grad_ref,
    packed_ref,
    residual_ref,
    table_ref,
    act_two_ref,
    mask_ref,
    old_sums_ref,
    residual_grad_ref,
    grad_two_ref,
    sums_ref,
    *refs,
    cols,
):
    *part_refs, total_ref, narrow_ref, columns_ref, part_ref = refs
    pixels, channels = residual_ref.shape
    block = min(CONV_ROWS, pixels)
    wide = jnp.float32
    mean, inverse, gain, shift = norm_rows(table_ref, 2)
    zeros = jnp.zeros((8, channels), wide)

    def input_grads(index, carry):
        rows = pl.ds(pl.multiple_of(index * block, block), block)
        normed_grad = lax.dot_general(
            packed_ref[rows, :], qkv_ref[...], (((1,), (1,)), ((), ())), preferred_element_type=wide
        )
        total_ref[rows, :] = normed_grad
        normed = (residual_ref[rows, :] - mean) * inverse
        return carry[0] + fold(normed_grad), carry[1] + fold(normed_grad * normed)

    sums = lax.fori_loop(0, pixels // block, input_grads, (zeros, zeros))
    sums_ref[...] = old_sums_ref[...]
    sums_ref[5:6, :] = column_total(sums[1])
    sums_ref[6:7, :] = column_total(sums[0])
    mean_grad, mean_cross = back_means(sums, gain, pixels)

    def finish(rows, carry):
        normed = (residual_ref[rows, :] - mean) * inverse
        back = inverse * (total_ref[rows, :] * gain - mean_grad - normed * mean_cross)
        total = grad_ref[rows, :].astype(wide) + back
        residual_grad_ref[rows, :] = total
        low = total.astype(jnp.bfloat16)
        grad_two_ref[rows, :] = low
        return carry + fold(low.astype(wide))

    sums_ref[7:8, :] = column_total(each_chunk(pixels, finish, zeros))
    weight_part(act_two_ref, grad_two_ref, mask_ref, narrow_ref, columns_ref, part_ref, cols)
    rows, width = part_refs[0].shape
    send_order(part_ref.at[0:rows, :], part_refs, 1, width)


def second_kernel(
    total_ref,
    partial_ref,
    middle_ref,
    table_ref,
    act_one_ref,
    mask_ref,
    old_sums_ref,
    grad_one_ref,
    sums_ref,
    *refs,
    cols,
):
    *part_refs, narrow_ref, columns_ref, part_ref = refs
    pixels, channels = middle_ref.shape
    sums = partial_ref[0:8, :], partial_ref[8:16, :]
    back = norm_back(total_ref, sums, lambda rows: middle_ref[rows, :], table_ref, 1)
    sums_ref[...] = old_sums_ref[...]
    sums_ref[2:3, :] = column_total(sums[1])
    sums_ref[3:4, :] = column_total(sums[0])

    def finish(rows, carry):
        low = back(rows).astype(jnp.bfloat16)
        grad_one_ref[rows, :] = low
        return carry + fold(low.astype(jnp.float32))

    zeros = jnp.zeros((8, channels), jnp.float32)
    sums_ref[4:5, :] = column_total(each_chunk(pixels, finish, zeros))
    weight_part(act_one_ref, grad_one_ref, mask_ref, narrow_ref, columns_ref, part_ref, cols)
    rows, width = part_refs[0].shape
    send_order(part_ref.at[0:rows, :], part_refs, 1, width)


def first_kernel(
    grad_one_ref,
    features_ref,
    residual_grad_ref,
    table_ref,
    mask_ref,
    old_sums_ref,
    weights_ref,
    input_grad_ref,
    sums_ref,
    taps_ref,
    total_ref,
    *,
    cols,
):
    def read(rows):
        return features_ref[rows, :].astype(jnp.float32)

    sums = conv_back(
        grad_one_ref, weights_ref.at[0], mask_ref, taps_ref, total_ref, read, table_ref, 0, cols
    )
    back = norm_back(total_ref, sums, read, table_ref, 0)
    sums_ref[...] = old_sums_ref[...]
    sums_ref[0:1, :] = column_total(sums[1])
    sums_ref[1:2, :] = column_total(sums[0])
    count = input_grad_ref.shape[0]
    own = pl.ds(pl.multiple_of(lax.axis_index("height") * count, count), count)
    input_grad_ref[...] = (residual_grad_ref[own, :] + back(own)).astype(jnp.bfloat16)


def blend_kernel(*refs):
    count = len(refs) // 3
    mixed, parts, joints = refs[:count], refs[count : 2 * count], refs[2 * count :]
    total = mixed[0][...].astype(jnp.float32)
    for piece in mixed[1:]:
        total = total + piece[...].astype(jnp.float32)
    total = total.astype(jnp.bfloat16)
    share, width = total.shape
    for part, joint in zip(parts, joints):
        for block in range(width // LANES):
            joint[block * share : (block + 1) * share, :] = total[
                :, block * LANES : (block + 1) * LANES
            ]
        joint[width // LANES * share :, :] = part[...]


def place_kernel(*refs):
    joints, (qkv_hbm, proj_hbm, packed_ref, qkv_ref, proj_ref, sems) = refs[:-6], refs[-6:]
    quarter, width = packed_ref.shape
    share = quarter // len(joints)
    me = lax.axis_index("canvas")
    for step, joint in enumerate(joints):
        place = pl.ds(pl.multiple_of((me ^ step) * share, share), share)
        for block in range(width // LANES):
            packed_ref[place, block * LANES : (block + 1) * LANES] = joint[
                block * share : (block + 1) * share, :
            ]
    spread_quarters([packed_ref], 0, qkv_ref, proj_ref, qkv_hbm, proj_hbm, sems)


def spread_quarters(packed, offset, qkv_ref, proj_ref, qkv_hbm, proj_hbm, sems):
    quarter = packed[0].shape[0]
    inner = qkv_ref.shape[2]
    copies = []
    for index, packed_ref in enumerate(packed):
        owner = own_quarter() ^ (index + offset)
        rows = pl.ds(pl.multiple_of(owner * quarter, quarter), quarter)
        qkv_ref[index] = packed_ref[:, 0:inner].astype(jnp.float32)
        proj_ref[index] = packed_ref[:, inner:].astype(jnp.float32)
        for which, (held, target) in enumerate(((qkv_ref, qkv_hbm), (proj_ref, proj_hbm))):
            copy = pltpu.make_async_copy(held.at[index], target.at[rows, :], sems.at[index, which])
            copy.start()
            copies.append(copy)
    for copy in copies:
        copy.wait()


def join_kernel(*refs):
    ins, (qkv_hbm, proj_hbm, conv_ref, qkv_ref, proj_ref, sems) = refs[:-6], refs[-6:]
    packed, ones, joints = ins[2:5], ins[5 : 5 + (len(ins) - 5) // 2], ins[5 + (len(ins) - 5) // 2 :]
    rows = ones[0].shape[0]
    for which, parts in enumerate((ones, joints)):
        total = jnp.zeros(ones[0].shape, jnp.float32)
        for part in parts:
            total = total + part[part.shape[0] - rows :, :].astype(jnp.float32)
        conv_ref[which] = total.reshape(conv_ref.shape[1:])
    spread_quarters(packed, 1, qkv_ref, proj_ref, qkv_hbm, proj_hbm, sems)


def sums_kernel(*refs):
    gains_ref, shifts_ref, conv_ref, qv_ref, proj_ref = refs[-5:]
    total = refs[0][...]
    for ref in refs[1:-5]:
        total = total + ref[...]
    for row, start in enumerate((0, 2, 5)):
        gains_ref[row : row + 1, :] = total[start : start + 1]
        shifts_ref[row : row + 1, :] = total[start + 1 : start + 2]
    conv_ref[0:1, :] = total[4:5]
    conv_ref[1:2, :] = total[7:8]
    qv_ref[...] = total[8:10]
    proj_ref[...] = total[10:11]


def call_kernel(kernel, outputs, scratch, operands, places, flops, limit, out_places=None, aliases={}):
    out_places = out_places or "v" * len(outputs)
    spaces = {
        "v": pl.BlockSpec(memory_space=pltpu.VMEM),
        "s": pl.BlockSpec(memory_space=pltpu.SMEM),
        "h": pl.BlockSpec(memory_space=pl.ANY),
        "o": pl.BlockSpec(memory_space=pltpu.VMEM),
        "a": pl.BlockSpec(memory_space=pl.ANY),
    }
    moved = sum(array.size * array.dtype.itemsize for array in operands)
    held = {"v": pltpu.VMEM, "h": pltpu.HBM, "o": jax.ShapeDtypeStruct}
    operands = [
        pltpu.with_memory_space_constraint(array, pltpu.HBM) if place == "h" else array
        for array, place in zip(operands, places)
    ]
    return pl.pallas_call(
        kernel,
        out_shape=[held[place](*output) for output, place in zip(outputs, out_places)],
        in_specs=[spaces[place] for place in places],
        out_specs=[spaces[place] for place in out_places],
        scratch_shapes=scratch,
        input_output_aliases=aliases,
        compiler_params=pltpu.CompilerParams(vmem_limit_bytes=limit * 2**20),
        cost_estimate=pl.CostEstimate(flops=flops, bytes_accessed=moved, transcendentals=0),
    )(*operands)


def send_height(block, step):
    size = lax.axis_size("height")
    return lax.ppermute(block, "height", [(i, i ^ step) for i in range(size)])


def send_chips(block):
    return [send_height(block, step) for step in range(2, lax.axis_size("height"), 2)]


def with_cores(blocks):
    return [piece for block in blocks for piece in (block, send_height(block, 1))]


def trade_canvas(pieces):
    size = lax.axis_size("canvas")
    return [pieces[0]] + [
        lax.ppermute(piece, "canvas", [(i, i ^ step) for i in range(size)])
        for step, piece in enumerate(pieces)
        if step
    ]


def whole_canvas(
    features,
    tile_ids,
    norm_gains,
    norm_shifts,
    conv_weights,
    conv_biases,
    qkv_weight,
    qv_bias,
    proj_weight,
    proj_bias,
    cotangent,
):
    height_size = lax.axis_size("height")
    canvas_size = lax.axis_size("canvas")
    local_rows, cols, channels = features.shape[1:]
    all_rows = tile_ids.shape[1]
    pixels = all_rows * cols
    own_pixels = local_rows * cols
    out_share = channels // height_size
    ci_share = channels // canvas_size
    quarter = channels // 4
    row_share = quarter // canvas_size
    low, wide = jnp.bfloat16, jnp.float32

    own_features = features.reshape(own_pixels, channels)
    own_grad = cotangent.reshape(own_pixels, channels)
    held_features = [own_features] + send_chips(own_features)
    pieces = with_cores(held_features)
    own_grad, *pieces[::2] = lax.optimization_barrier((own_grad, *held_features))
    held_grads = [own_grad] + send_chips(own_grad)

    plane = ((pixels, channels), low)
    plane_wide = ((pixels, channels), wide)
    sums_shape = ((16, channels), wide)
    part_shapes = [((9 * out_share, ci_share), low)] * canvas_size
    mixed_shapes = [((row_share, 4 * channels), low)] * canvas_size
    taps = pltpu.VMEM((pixels + 2 * cols, 3 * channels), low)
    held_wide = pltpu.VMEM((pixels, channels), wide)
    flipped = pltpu.VMEM((channels, pixels), low)
    narrow = pltpu.VMEM((pixels + 2 * cols, 3 * NARROW), wide)
    columns = pltpu.VMEM((pixels, 5 * NARROW), low)
    part_held = pltpu.VMEM((5 * NARROW, channels), low)
    sem = pltpu.SemaphoreType.DMA
    conv_flops = 2 * 9 * pixels * channels * channels
    dot_flops = 2 * pixels * channels * channels
    score_flops = 2 * pixels * pixels * channels
    scale = channels ** (-0.5)

    (
        all_features,
        act_one,
        middle,
        act_two,
        residual,
        table,
        mask,
        id_rows,
        id_cols,
        turned,
        held_qkv,
        held_proj,
    ) = call_kernel(
        functools.partial(conv_kernel, cols=cols, count=height_size),
        [
            plane,
            plane,
            plane_wide,
            plane,
            plane_wide,
            ((16, channels), wide),
            ((2, pixels, LANES), wide),
            ((pixels, LANES), jnp.int32),
            ((8, pixels), jnp.int32),
            ((2, 3, channels, 3 * channels), low),
            (qkv_weight.shape, low),
            (proj_weight.shape, low),
        ],
        [
            pltpu.SMEM(tile_ids.shape, jnp.int32),
            pltpu.VMEM(norm_gains.shape, wide),
            pltpu.VMEM(norm_shifts.shape, wide),
            pltpu.VMEM(conv_biases.shape, wide),
            pltpu.VMEM(conv_weights.shape, low),
            taps,
            sem((26,)),
            sem((height_size,)),
        ],
        [
            *pieces,
            tile_ids,
            norm_gains,
            norm_shifts,
            conv_biases,
            conv_weights,
            qkv_weight,
            proj_weight,
        ],
        "h" + "a" * (height_size - 1) + "h" * 7,
        2 * conv_flops,
        24,
    )
    residual, *held_grads = lax.optimization_barrier((residual, *held_grads))
    grad_pieces = with_cores(held_grads)
    normed, query, key, value, soft, out_flip, output = call_kernel(
        functools.partial(score_kernel, score_scale=scale),
        [
            plane,
            plane,
            plane,
            plane,
            ((pixels, pixels), low),
            ((channels, pixels), low),
            ((own_pixels, channels), low),
        ],
        [
            pltpu.VMEM(qv_bias.shape, wide),
            pltpu.VMEM((1, channels), wide),
            flipped,
            sem((2,)),
        ],
        [
            qv_bias,
            proj_bias.reshape(1, channels),
            held_qkv,
            held_proj,
            residual,
            table,
            id_rows,
            id_cols,
        ],
        "hhvvvvvv",
        3 * dot_flops + 2 * score_flops,
        16,
        "v" * 6 + "o",
    )
    normed, *grad_pieces = lax.optimization_barrier((normed, *grad_pieces))
    all_grad, packed, sums, *mixed = call_kernel(
        functools.partial(attention_kernel, score_scale=scale, count=height_size),
        [plane, ((pixels, 3 * channels), low), sums_shape, *mixed_shapes],
        [
            pltpu.VMEM((quarter, 4 * channels), low),
            flipped,
            held_wide,
            held_wide,
            pltpu.VMEM((quarter, pixels), low),
            sem((height_size,)),
        ],
        [held_proj, normed, query, key, value, soft, out_flip, *grad_pieces],
        "vvvvvvvh" + "a" * (height_size - 1),
        3 * dot_flops + 4 * score_flops,
        20,
    )
    mixed = trade_canvas(mixed)
    residual_grad, grad_two, sums, *parts_two = call_kernel(
        functools.partial(third_kernel, cols=cols),
        [plane_wide, plane, sums_shape, *part_shapes],
        [
            held_wide,
            narrow,
            columns,
            part_held,
        ],
        [held_qkv, all_grad, packed, residual, table, act_two, mask, sums],
        "vvvvvvvv",
        3 * dot_flops + conv_flops // height_size,
        16,
    )
    joint_shape = (row_share * 4 * channels // LANES + 9 * out_share, LANES)
    joints = call_kernel(
        blend_kernel,
        [(joint_shape, low)] * canvas_size,
        [],
        mixed + parts_two,
        "v" * 2 * canvas_size,
        0,
        12,
    )
    joints = trade_canvas(joints)
    act_two_grad, partial_sums = call_kernel(
        functools.partial(turn_kernel, cols=cols),
        [plane_wide, sums_shape],
        [taps],
        [grad_two, mask, turned, middle, table],
        "vvvvv",
        conv_flops,
        16,
    )
    grad_one, sums, *parts_one = call_kernel(
        functools.partial(second_kernel, cols=cols),
        [plane, sums_shape, *part_shapes],
        [narrow, columns, part_held],
        [act_two_grad, partial_sums, middle, table, act_one, mask, sums],
        "vvvvvvv",
        conv_flops // height_size,
        16,
    )
    parts_one = trade_canvas(parts_one)
    grad_one, *joints = lax.optimization_barrier((grad_one, *joints))
    qkv_grad, proj_grad, own_mixed = call_kernel(
        place_kernel,
        [(qkv_weight.shape, wide), (proj_weight.shape, wide), ((quarter, 4 * channels), low)],
        [
            pltpu.VMEM((1, quarter, 3 * channels), wide),
            pltpu.VMEM((1, quarter, channels), wide),
            sem((1, 2)),
        ],
        joints,
        "v" * canvas_size,
        0,
        12,
        "hhv",
    )
    chip_mixed = send_height(own_mixed, 2)
    core_mixed = send_height(own_mixed, 1)
    input_grad, sums = call_kernel(
        functools.partial(first_kernel, cols=cols),
        [((own_pixels, channels), low), sums_shape],
        [taps, held_wide],
        [grad_one, all_features, residual_grad, table, mask, sums, turned],
        "vvvvvvv",
        conv_flops,
        16,
        "ov",
    )
    sums, chip_mixed, core_mixed, *parts_one = lax.optimization_barrier(
        (sums, chip_mixed, core_mixed, *parts_one)
    )
    both_mixed = send_height(chip_mixed, 1)
    all_sums = trade_canvas([sums] * canvas_size)
    qkv_grad, proj_grad, conv_grad = call_kernel(
        join_kernel,
        [
            (qkv_weight.shape, wide),
            (proj_weight.shape, wide),
            ((2, 3, 3, out_share, ci_share), wide),
        ],
        [
            pltpu.VMEM((3, quarter, 3 * channels), wide),
            pltpu.VMEM((3, quarter, channels), wide),
            sem((3, 2)),
        ],
        [qkv_grad, proj_grad, chip_mixed, core_mixed, both_mixed, *parts_one, *joints],
        "hhvvv" + "v" * (2 * canvas_size),
        0,
        12,
        "hho",
        {0: 0, 1: 1},
    )
    vector_shapes = [norm_gains.shape, norm_shifts.shape, conv_biases.shape, qv_bias.shape]
    gains_grad, shifts_grad, biases_grad, qv_grad, proj_bias_grad = call_kernel(
        sums_kernel,
        [(shape, wide) for shape in vector_shapes + [(1, channels)]],
        [],
        all_sums,
        "v" * canvas_size,
        0,
        16,
        "ooooo",
    )
    own_shape = (1, local_rows, cols, channels)
    return (
        output.reshape(own_shape),
        input_grad.reshape(own_shape),
        gains_grad,
        shifts_grad,
        jnp.swapaxes(conv_grad, 3, 4),
        biases_grad,
        qkv_grad,
        qv_grad,
        proj_grad,
        proj_bias_grad.reshape(channels),
    )


def on_device(*arrays):
    features, tile_ids = arrays[0], arrays[1]
    local_rows, cols, channels = features.shape[1:]
    pixels = tile_ids.shape[1] * cols
    height_size, canvas_size = lax.axis_size("height"), lax.axis_size("canvas")
    powers = all(size & (size - 1) == 0 for size in (height_size, canvas_size, cols))
    fits = (
        powers
        and height_size > 2
        and channels == LANES * canvas_size
        and pixels <= MOST_PIXELS
        and pixels % min(CONV_ROWS, pixels) == 0
        and pixels % FILL_ROWS == 0
        and FILL_ROWS % CHUNK == 0
        and (local_rows * cols) % LANES == 0
        and CHUNK % cols == 0
        and cols % 16 == 0
        and channels % (LANES * canvas_size) == 0
        and 2 * channels == NARROW * height_size
    )
    return whole_canvas(*arrays) if fits else split_canvas(*arrays)


def solution(mesh):
    in_specs = (
        P("canvas", "height", None, None),
        P("canvas", None),
        P(),
        P(),
        P(),
        P(),
        P(),
        P(),
        P(),
        P(),
        P("canvas", "height", None, None),
    )
    out_specs = (
        P("canvas", "height", None, None),
        P("canvas", "height", None, None),
        P(),
        P(),
        P(None, None, None, "canvas", "height"),
        P(),
        P(),
        P(),
        P(),
        P(),
    )
    return jax.shard_map(
        on_device, mesh=mesh, in_specs=in_specs, out_specs=out_specs, check_vma=False
    )
```

```python
import functools

import jax
import jax.numpy as jnp
from jax import lax
from jax.experimental import pallas as pl
from jax.experimental.pallas import tpu as pltpu
from jax.sharding import PartitionSpec as P

GROUPS = 32


epsilon = 1e-06
masked_score = -1e30
MOST_PIXELS = 1024
LANES = 128
NARROW = 128
CHUNK = 128
CONV_ROWS = 1024
FILL_ROWS = 256
QUERY_ROWS = 512


def extended(block, sides, width):
    for axis, dim in sides:
        count = lax.axis_size(axis)
        forward = [(i, i + 1) for i in range(count - 1)]
        backward = [(target, source) for source, target in forward]
        low = lax.ppermute(
            lax.slice_in_dim(block, block.shape[dim] - width, None, axis=dim), axis, forward
        )
        high = lax.ppermute(lax.slice_in_dim(block, 0, width, axis=dim), axis, backward)
        block = jnp.concatenate([low, block, high], axis=dim)
    return block


def group_total(vector):
    return vector.reshape(GROUPS, -1).sum(axis=1)


def spread_groups(vector, channels):
    return jnp.repeat(vector, channels // GROUPS)


def norm_forward(values, gain, shift, members):
    channels = values.shape[1]
    totals = lax.psum(group_total(jnp.sum(values, axis=0)), "height")
    centered = values - spread_groups(totals / members, channels)
    squares = lax.psum(group_total(jnp.sum(centered * centered, axis=0)), "height")
    inverse = spread_groups(lax.rsqrt(squares / members + epsilon), channels)
    normed = centered * inverse
    return (normed, inverse, normed * gain + shift)


def norm_backward(grad_in, normed, inverse, gain, members):
    channels = grad_in.shape[1]
    scaled = grad_in * gain
    both_sums = lax.psum(
        (group_total(jnp.sum(scaled, axis=0)), group_total(jnp.sum(scaled * normed, axis=0))),
        "height",
    )
    mean_grad = spread_groups(both_sums[0] / members, channels)
    mean_cross = spread_groups(both_sums[1] / members, channels)
    result = inverse * (scaled - mean_grad - normed * mean_cross)
    return (result, jnp.sum(grad_in * normed, axis=0), jnp.sum(grad_in, axis=0))


def swish(values):
    return values * jax.nn.sigmoid(values)


def swish_slope(values):
    sigmoid_part = jax.nn.sigmoid(values)
    return sigmoid_part * (1.0 + values * (1.0 - sigmoid_part))


def tap_columns(padded, row_mask, local_rows, canvas_cols):
    pieces = []
    for row_tap in range(3):
        rows_taken = padded[row_tap : row_tap + local_rows] * row_mask[:, row_tap, None, None]
        for col_tap in range(3):
            pieces.append(rows_taken[:, col_tap : col_tap + canvas_cols])
    stacked = jnp.concatenate(pieces, axis=2)
    return stacked.reshape(local_rows * canvas_cols, stacked.shape[2])


def conv_forward(acts, row_mask, weight, bias):
    local_rows, canvas_cols, channels = acts.shape
    rimmed = extended(acts, (("height", 0),), 1)
    padded = jnp.pad(rimmed, ((0, 0), (1, 1), (0, 0)))
    gathered = tap_columns(padded, row_mask, local_rows, canvas_cols)
    result = (
        jnp.dot(
            gathered, weight.reshape(9 * channels, channels), preferred_element_type=jnp.float32
        )
        + bias
    )
    return (result, gathered)


def conv_backward(grad_low, row_mask, weight, gathered):
    local_rows, canvas_cols, channels = grad_low.shape
    flat_grad = grad_low.reshape(local_rows * canvas_cols, channels)
    weight_grad = lax.dot_general(
        gathered, flat_grad, (((0,), (0,)), ((), ())), preferred_element_type=jnp.float32
    )
    rimmed = extended(grad_low, (("height", 0),), 1)
    padded = jnp.pad(rimmed, ((0, 0), (1, 1), (0, 0)))
    grad_taps = tap_columns(padded, row_mask, local_rows, canvas_cols)
    flipped = jnp.transpose(weight[::-1, ::-1], (0, 1, 3, 2)).reshape(9 * channels, channels)
    input_part = jnp.dot(grad_taps, flipped, preferred_element_type=jnp.float32)
    return (
        input_part,
        weight_grad.reshape(3, 3, channels, channels),
        jnp.sum(flat_grad.astype(jnp.float32), axis=0),
    )


def take_rows(array, offset, count):
    return lax.dynamic_slice_in_dim(array, offset, count)


def score_grads(
    queries, out_grad, log_total, row_dots, query_ids, key_rows, value_rows, key_ids, score_scale
):
    scores = (
        lax.dot_general(
            queries, key_rows, (((1,), (1,)), ((), ())), preferred_element_type=jnp.float32
        )
        * score_scale
    )
    same_tile = query_ids[:, None] == key_ids[None, :]
    softmax_block = jnp.exp(jnp.where(same_tile, scores - log_total[:, None], masked_score))
    weight_grad = lax.dot_general(
        out_grad, value_rows, (((1,), (1,)), ((), ())), preferred_element_type=jnp.float32
    )
    score_grad = (softmax_block * (weight_grad - row_dots[:, None])).astype(jnp.bfloat16)
    return (softmax_block.astype(jnp.bfloat16), score_grad)


def split_canvas(
    features,
    tile_ids,
    norm_gains,
    norm_shifts,
    conv_weights,
    conv_biases,
    qkv_weight,
    qv_bias,
    proj_weight,
    proj_bias,
    cotangent,
):
    height_size = lax.axis_size("height")
    local_rows = features.shape[1]
    canvas_cols = features.shape[2]
    channels = features.shape[3]
    pixels = local_rows * canvas_cols
    row_ids = tile_ids[0]
    all_rows = row_ids.shape[0]
    members = float(all_rows * canvas_cols * (channels // GROUPS))
    score_scale = channels ** (-0.5)
    first_row = lax.axis_index("height") * local_rows
    edge_ids = jnp.full((1,), -1, jnp.int32)
    padded_ids = jnp.concatenate([edge_ids, row_ids, edge_ids])
    near_ids = lax.dynamic_slice_in_dim(padded_ids, first_row, local_rows + 2)
    own_rows = near_ids[1 : local_rows + 1]
    row_mask = jnp.stack(
        [near_ids[row_tap : row_tap + local_rows] == own_rows for row_tap in range(3)], axis=1
    ).astype(jnp.bfloat16)
    key_ids = jnp.repeat(row_ids, canvas_cols)
    query_ids = jnp.repeat(own_rows, canvas_cols)
    grid_shape = (local_rows, canvas_cols, channels)
    inputs = features[0].reshape(pixels, channels).astype(jnp.float32)
    normed_one, inverse_one, pre_one = norm_forward(inputs, norm_gains[0], norm_shifts[0], members)
    act_one = swish(pre_one).astype(jnp.bfloat16).reshape(grid_shape)
    middle, taps_one = conv_forward(act_one, row_mask, conv_weights[0], conv_biases[0])
    normed_two, inverse_two, pre_two = norm_forward(middle, norm_gains[1], norm_shifts[1], members)
    act_two = swish(pre_two).astype(jnp.bfloat16).reshape(grid_shape)
    branch, taps_two = conv_forward(act_two, row_mask, conv_weights[1], conv_biases[1])
    residual = inputs + branch
    normed_three, inverse_three, pre_three = norm_forward(
        residual, norm_gains[2], norm_shifts[2], members
    )
    attn_input = pre_three.astype(jnp.bfloat16)
    mixed = jnp.dot(attn_input, qkv_weight, preferred_element_type=jnp.float32)
    queries = (mixed[:, :channels] + qv_bias[0]).astype(jnp.bfloat16)
    key_rows = mixed[:, channels : 2 * channels].astype(jnp.bfloat16)
    value_rows = (mixed[:, 2 * channels :] + qv_bias[1]).astype(jnp.bfloat16)
    running_max = jnp.full((pixels,), masked_score, jnp.float32)
    key_piece = lax.all_gather(key_rows, "height", axis=0, tiled=True)
    value_piece = lax.all_gather(value_rows, "height", axis=0, tiled=True)
    scores = (
        lax.dot_general(
            queries, key_piece, (((1,), (1,)), ((), ())), preferred_element_type=jnp.float32
        )
        * score_scale
    )
    same_tile = query_ids[:, None] == key_ids[None, :]
    scores = jnp.where(same_tile, scores, masked_score)
    new_max = jnp.maximum(running_max, jnp.max(scores, axis=1))
    weights = jnp.where(same_tile, jnp.exp(scores - new_max[:, None]), 0.0)
    summed_out = jnp.dot(
        weights.astype(jnp.bfloat16), value_piece, preferred_element_type=jnp.float32
    )
    total_weight = jnp.sum(weights, axis=1)
    log_total = new_max + jnp.log(total_weight)
    attended = summed_out / total_weight[:, None]
    attended_low = attended.astype(jnp.bfloat16)
    output = (
        residual
        + jnp.dot(attended_low, proj_weight, preferred_element_type=jnp.float32)
        + proj_bias
    )
    out_grad = cotangent[0].reshape(pixels, channels)
    out_grad_full = out_grad.astype(jnp.float32)
    proj_grad = lax.dot_general(
        attended_low, out_grad, (((0,), (0,)), ((), ())), preferred_element_type=jnp.float32
    )
    proj_bias_grad = jnp.sum(out_grad_full, axis=0)
    attended_grad = lax.dot_general(
        out_grad, proj_weight, (((1,), (1,)), ((), ())), preferred_element_type=jnp.float32
    ).astype(jnp.bfloat16)
    row_dots = jnp.sum(attended_grad.astype(jnp.float32) * attended, axis=1)
    block_rows = pixels * min(height_size, 8)
    zero_block = jnp.zeros((pixels, channels), jnp.float32)
    key_all, value_all = (
        lax.all_gather(key_rows, "height", axis=0, tiled=True),
        lax.all_gather(value_rows, "height", axis=0, tiled=True),
    )
    query_all, grad_all = (
        lax.all_gather(queries, "height", axis=0, tiled=True),
        lax.all_gather(attended_grad, "height", axis=0, tiled=True),
    )
    total_all, dots_all = (
        lax.all_gather(log_total, "height", axis=0, tiled=True),
        lax.all_gather(row_dots, "height", axis=0, tiled=True),
    )

    def own_query_step(running, block_index):
        offset = block_index * block_rows
        key_part = take_rows(key_all, offset, block_rows)
        rounded, score_grad = score_grads(
            queries,
            attended_grad,
            log_total,
            row_dots,
            query_ids,
            key_part,
            take_rows(value_all, offset, block_rows),
            take_rows(key_ids, offset, block_rows),
            score_scale,
        )
        return (
            running
            + jnp.dot(score_grad, key_part, preferred_element_type=jnp.float32) * score_scale,
            None,
        )

    def own_key_step(running, block_index):
        offset = block_index * block_rows
        query_part = take_rows(query_all, offset, block_rows)
        grad_part = take_rows(grad_all, offset, block_rows)
        rounded, score_grad = score_grads(
            query_part,
            grad_part,
            take_rows(total_all, offset, block_rows),
            take_rows(dots_all, offset, block_rows),
            take_rows(key_ids, offset, block_rows),
            key_rows,
            value_rows,
            query_ids,
            score_scale,
        )
        key_part = (
            lax.dot_general(
                score_grad, query_part, (((0,), (0,)), ((), ())), preferred_element_type=jnp.float32
            )
            * score_scale
        )
        value_part = lax.dot_general(
            rounded, grad_part, (((0,), (0,)), ((), ())), preferred_element_type=jnp.float32
        )
        return ((running[0] + key_part, running[1] + value_part), None)

    block_count = key_all.shape[0] // block_rows
    query_grad, unused_one = lax.scan(own_query_step, zero_block, jnp.arange(block_count))
    (key_grad, value_grad), unused_two = lax.scan(
        own_key_step, (zero_block, zero_block), jnp.arange(block_count)
    )
    query_low = query_grad.astype(jnp.bfloat16)
    key_low = key_grad.astype(jnp.bfloat16)
    value_low = value_grad.astype(jnp.bfloat16)
    stacked_grad = jnp.concatenate([query_low, key_low, value_low], axis=1)
    qkv_grad = lax.dot_general(
        attn_input, stacked_grad, (((0,), (0,)), ((), ())), preferred_element_type=jnp.float32
    )
    qv_grad = jnp.stack(
        [
            jnp.sum(query_low.astype(jnp.float32), axis=0),
            jnp.sum(value_low.astype(jnp.float32), axis=0),
        ]
    )
    normed_grad = lax.dot_general(
        stacked_grad, qkv_weight, (((1,), (1,)), ((), ())), preferred_element_type=jnp.float32
    )
    back_three, gain_three, shift_three = norm_backward(
        normed_grad, normed_three, inverse_three, norm_gains[2], members
    )
    residual_grad = out_grad_full + back_three
    grad_two = residual_grad.astype(jnp.bfloat16).reshape(grid_shape)
    act_two_grad, weight_two_grad, bias_two_grad = conv_backward(
        grad_two, row_mask, conv_weights[1], taps_two
    )
    middle_grad, gain_two, shift_two = norm_backward(
        act_two_grad * swish_slope(pre_two), normed_two, inverse_two, norm_gains[1], members
    )
    grad_one = middle_grad.astype(jnp.bfloat16).reshape(grid_shape)
    act_one_grad, weight_one_grad, bias_one_grad = conv_backward(
        grad_one, row_mask, conv_weights[0], taps_one
    )
    input_back, gain_one, shift_one = norm_backward(
        act_one_grad * swish_slope(pre_one), normed_one, inverse_one, norm_gains[0], members
    )
    input_grad = residual_grad + input_back
    conv_grad = jnp.stack([weight_one_grad, weight_two_grad])
    conv_part = lax.psum_scatter(conv_grad, "height", scatter_dimension=4, tiled=True)
    conv_part = lax.psum_scatter(
        conv_part.astype(jnp.bfloat16), "canvas", scatter_dimension=3, tiled=True
    ).astype(jnp.float32)
    summed = lax.psum(
        (
            jnp.stack([gain_one, gain_two, gain_three]),
            jnp.stack([shift_one, shift_two, shift_three]),
            jnp.stack([bias_one_grad, bias_two_grad]),
            qkv_grad,
            qv_grad,
            proj_grad,
            proj_bias_grad,
        ),
        ("canvas", "height"),
    )
    return (
        output.astype(jnp.bfloat16).reshape((1,) + grid_shape),
        input_grad.astype(jnp.bfloat16).reshape((1,) + grid_shape),
        summed[0],
        summed[1],
        conv_part,
        summed[2],
        summed[3],
        summed[4],
        summed[5],
        summed[6],
    )


def fold(block):
    rows, width = block.shape
    return jnp.sum(block.reshape(rows // 8, 8, width), axis=0)


def group_lanes(block, group):
    lane = lax.broadcasted_iota(jnp.int32, block.shape, 1)
    width = block.shape[1]
    step = 1
    while step < group:
        above = pltpu.roll(block, step, 1)
        below = pltpu.roll(block, width - step, 1)
        block = block + jnp.where((lane & step) != 0, above, below)
        step *= 2
    return block


def group_mean(partial, members):
    spread = group_lanes(partial, partial.shape[1] // GROUPS)
    return jnp.sum(spread, axis=0, keepdims=True) * (1.0 / members)


def widen(block, width):
    return jnp.concatenate([block] * (width // block.shape[1]), axis=1)


def each_chunk(pixels, body, carry):
    for start in range(0, pixels, CHUNK):
        carry = body(pl.ds(start, CHUNK), carry)
    return carry


def aligned(start, step):
    return start if isinstance(start, int) else pl.multiple_of(start, step)


def fold_about(block, center):
    rows, width = block.shape
    offset = block.reshape(rows // 8, 8, width) - center[None]
    return jnp.sum(offset, axis=0), jnp.sum(offset * offset, axis=0)


def finish_stats(center, sums, squares, pixels):
    width = center.shape[1] // GROUPS
    share = pixels / 8.0
    means = center + sums * (1.0 / share)
    spread = squares - sums * sums * (1.0 / share)
    mean = group_mean(means, 8.0 * width)
    offset = means - mean
    variance = group_mean(spread + share * offset * offset, float(pixels * width))
    return mean, lax.rsqrt(variance + epsilon)


class RunningStats:
    def __init__(self):
        self.center = None

    def add(self, block):
        if self.center is None:
            self.center = block[0:8]
            self.sums, self.squares = fold_about(block, self.center)
        else:
            sums, squares = fold_about(block, self.center)
            self.sums, self.squares = self.sums + sums, self.squares + squares

    def finish(self, pixels):
        return finish_stats(self.center, self.sums, self.squares, pixels)


def put_taps(taps_ref, block, rows, cols):
    count, channels = block.shape
    place = lax.broadcasted_iota(jnp.int32, block.shape, 0) & (cols - 1)
    left = jnp.where(place == 0, 0.0, pltpu.roll(block, 1, 0))
    right = jnp.where(place == cols - 1, 0.0, pltpu.roll(block, count - 1, 0))
    inner = pl.ds(aligned(rows.start + cols, cols), count)
    taps_ref[inner, 0:channels] = left.astype(jnp.bfloat16)
    taps_ref[inner, channels : 2 * channels] = block.astype(jnp.bfloat16)
    taps_ref[inner, 2 * channels :] = right.astype(jnp.bfloat16)


def clear_edges(taps_ref, cols):
    edge = jnp.zeros((cols, taps_ref.shape[1]), taps_ref.dtype)
    taps_ref[0:cols, :] = edge
    taps_ref[taps_ref.shape[0] - cols :, :] = edge


def run_conv(taps_ref, product, mask_ref, total_ref, fill, first, last, cols):
    pixels, channels = total_ref.shape
    for start in range(0, pixels, FILL_ROWS):
        for inner in range(start, start + FILL_ROWS, CHUNK):
            fill(pl.ds(inner, CHUNK))
        rows = pl.ds(start, FILL_ROWS)
        total_ref[rows, :] = first(rows, product(taps_ref, pl.ds(start + cols, FILL_ROWS), 1))
    block = min(CONV_ROWS, pixels)
    for row_tap in (0, 2):
        for start in range(0, pixels, block):
            rows = pl.ds(start, block)
            part = product(taps_ref, pl.ds(start + row_tap * cols, block), row_tap)
            mask = widen(mask_ref[row_tap // 2, rows, :], channels)
            value = total_ref[rows, :] + mask * part
            total_ref[rows, :] = value if row_tap == 0 else last(rows, value)


def product_forward(weight_ref):
    channels = weight_ref.shape[-1]

    def product(taps_ref, shifted, row_tap):
        return jnp.dot(
            taps_ref[shifted, :],
            weight_ref[row_tap].reshape(3 * channels, channels),
            preferred_element_type=jnp.float32,
        )

    return product


def product_backward(weight_ref):
    def product(taps_ref, shifted, row_tap):
        return lax.dot_general(
            taps_ref[shifted, :],
            weight_ref[row_tap],
            (((1,), (1,)), ((), ())),
            preferred_element_type=jnp.float32,
        )

    return product


def smooth(values):
    part = 0.5 * jnp.tanh(0.5 * values) + 0.5
    return values * part, part


def activation(read, mean, inverse, gain, shift, act_ref, taps_ref, cols):
    scale = inverse * gain

    def fill(rows):
        act = smooth((read(rows) - mean) * scale + shift)[0]
        act_ref[rows, :] = act.astype(jnp.bfloat16)
        put_taps(taps_ref, act, rows, cols)

    return fill


def back_means(sums, gain, pixels):
    channels = gain.shape[1]
    members = float(pixels * (channels // GROUPS))
    return group_mean(sums[0] * gain, members), group_mean(sums[1] * gain, members)


def column_total(partial):
    return jnp.sum(partial, axis=0, keepdims=True)


def weight_part(act_ref, grad_ref, mask_ref, narrow_ref, columns_ref, part_ref, cols):
    pixels, channels = act_ref.shape
    height = lax.axis_index("height")
    share = NARROW // 2
    block = pl.ds(pl.multiple_of((height // 2) * NARROW, NARROW), NARROW)
    parity = height % 2
    edge = jnp.zeros((cols, 3 * NARROW), jnp.float32)
    narrow_ref[0:cols, :] = edge
    narrow_ref[cols + pixels :, :] = edge

    def spread(rows, carry):
        own = grad_ref[rows, block].astype(jnp.float32)
        half = lax.broadcasted_iota(jnp.int32, own.shape, 1) // share
        turned = pltpu.roll(own, share, 1)
        both = jnp.where(half == parity, own, turned)
        place = lax.broadcasted_iota(jnp.int32, own.shape, 0) & (cols - 1)
        left = jnp.where(place == 0, 0.0, pltpu.roll(both, 1, 0))
        right = jnp.where(place == cols - 1, 0.0, pltpu.roll(both, CHUNK - 1, 0))
        inner = pl.ds(aligned(rows.start + cols, cols), CHUNK)
        narrow_ref[inner, 0:NARROW] = left
        narrow_ref[inner, NARROW : 2 * NARROW] = both
        narrow_ref[inner, 2 * NARROW :] = right
        return carry

    each_chunk(pixels, spread, 0)

    def gather(rows, carry):
        taps = []
        for row_tap in range(3):
            for col_tap in range(3):
                row_back, col_back = 2 - row_tap, 2 - col_tap
                shifted = pl.ds(aligned(rows.start + row_back * cols, cols), CHUNK)
                block = narrow_ref[shifted, col_back * NARROW : (col_back + 1) * NARROW]
                if row_back != 1:
                    block = block * mask_ref[row_back // 2, rows, :]
                taps.append(block)
        lower = lax.broadcasted_iota(jnp.int32, taps[0].shape, 1) < share
        for pair in range(5):
            second = taps[min(2 * pair + 1, 8)]
            columns_ref[rows, pair * NARROW : (pair + 1) * NARROW] = jnp.where(
                lower, taps[2 * pair], second
            ).astype(jnp.bfloat16)
        return carry

    each_chunk(pixels, gather, 0)
    part_ref[...] = lax.dot_general(
        columns_ref[...],
        act_ref[...],
        (((0,), (0,)), ((), ())),
        preferred_element_type=jnp.float32,
    ).astype(jnp.bfloat16)


def conv_back(grad_ref, weights_ref, mask_ref, taps_ref, total_ref, read, table_ref, which, cols):
    clear_edges(taps_ref, cols)
    mean, inverse, gain, shift = norm_rows(table_ref, which)
    sums = []

    def fill(rows):
        put_taps(taps_ref, grad_ref[rows, :].astype(jnp.float32), rows, cols)

    def slope(rows, value):
        normed = (read(rows) - mean) * inverse
        pre = normed * gain + shift
        part = smooth(pre)[1]
        grad = value * (part * (1.0 + pre * (1.0 - part)))
        sums.append((fold(grad), fold(grad * normed)))
        return grad

    run_conv(
        taps_ref,
        product_backward(weights_ref),
        mask_ref,
        total_ref,
        fill,
        lambda rows, part: part,
        slope,
        cols,
    )
    return sum(pair[0] for pair in sums), sum(pair[1] for pair in sums)


def norm_back(total_ref, sums, read, table_ref, which):
    mean, inverse, gain, shift = norm_rows(table_ref, which)
    mean_grad, mean_cross = back_means(sums, gain, total_ref.shape[0])

    def back(rows):
        normed = (read(rows) - mean) * inverse
        return inverse * (total_ref[rows, :] * gain - mean_grad - normed * mean_cross)

    return back


def turn_kernel(
    grad_ref, mask_ref, weights_ref, middle_ref, table_ref, total_ref, sums_ref, taps_ref, *, cols
):
    sums_ref[0:8, :], sums_ref[8:16, :] = conv_back(
        grad_ref,
        weights_ref.at[1],
        mask_ref,
        taps_ref,
        total_ref,
        lambda rows: middle_ref[rows, :],
        table_ref,
        1,
        cols,
    )


def norm_rows(table_ref, which):
    picks = (2 * which, 2 * which + 1, 6 + which, 9 + which)
    return tuple(table_ref[pick : pick + 1, :] for pick in picks)


def build_masks(ids_ref, mask_ref, id_rows_ref, id_cols_ref, cols):
    rows = ids_ref.shape[1]
    for row in range(rows):
        here = ids_ref[0, row]
        place = slice(row * cols, (row + 1) * cols)
        id_rows_ref[place, :] = jnp.full((cols, LANES), here, jnp.int32)
        for side, other in ((0, row - 1), (1, row + 1)):
            same = jnp.float32(0.0)
            if 0 <= other < rows:
                same = jnp.where(ids_ref[0, other] == here, 1.0, 0.0).astype(jnp.float32)
            mask_ref[side, place, :] = jnp.full((cols, LANES), same, jnp.float32)
    lane = lax.broadcasted_iota(jnp.int32, (8, LANES), 1)
    each = LANES // cols
    for block in range(rows // each):
        ids = jnp.full((8, LANES), ids_ref[0, block * each], jnp.int32)
        for step in range(1, each):
            ids = jnp.where(lane >= step * cols, ids_ref[0, block * each + step], ids)
        id_cols_ref[:, block * LANES : (block + 1) * LANES] = ids


def place_pieces(pieces, whole_ref, sems):
    own_pixels = whole_ref.shape[0] // len(pieces)
    height = lax.axis_index("height")
    copies = []
    for place, piece in enumerate(pieces):
        start = pl.multiple_of((height ^ place) * own_pixels, own_pixels)
        rows = pl.ds(start, own_pixels)
        copies.append(pltpu.make_async_copy(piece, whole_ref.at[rows, :], sems.at[place]))
    return copies


def conv_kernel(*refs, cols, count):
    pieces, refs = refs[:count], refs[count:]
    (
        ids_hbm,
        gains_hbm,
        shifts_hbm,
        biases_hbm,
        weights_hbm,
        qkv_hbm,
        proj_hbm,
        features_ref,
        act_one_ref,
        middle_ref,
        act_two_ref,
        residual_ref,
        table_ref,
        mask_ref,
        id_rows_ref,
        id_cols_ref,
        turned_ref,
        qkv_ref,
        proj_ref,
        ids_ref,
        gains_ref,
        shifts_ref,
        biases_ref,
        weights_ref,
        taps_ref,
        own_ref,
        sems,
        piece_sem,
    ) = refs
    pixels, channels = features_ref.shape
    wide = jnp.float32
    turned = [
        (
            weights_hbm.at[which, 2 - row_tap, 2 - col_tap],
            turned_ref.at[which, row_tap, :, col_tap * channels : (col_tap + 1) * channels],
        )
        for which in (1, 0)
        for row_tap in range(3)
        for col_tap in range(3)
    ]
    moves = [
        (ids_hbm, ids_ref),
        (gains_hbm, gains_ref),
        (shifts_hbm, shifts_ref),
        (weights_hbm.at[0], weights_ref.at[0]),
        (biases_hbm, biases_ref),
        (weights_hbm.at[1], weights_ref.at[1]),
        (qkv_hbm, qkv_ref),
        (proj_hbm, proj_ref),
    ] + turned
    copies = [
        pltpu.make_async_copy(source, target, sems.at[index])
        for index, (source, target) in enumerate(moves)
    ]
    own_copy = pltpu.make_async_copy(pieces[0], own_ref, piece_sem)
    for copy in [own_copy] + copies[:6]:
        copy.start()
    clear_edges(taps_ref, cols)

    def read_input(rows):
        return features_ref[rows, :].astype(wide)

    def read_middle(rows):
        return middle_ref[rows, :]

    height = lax.axis_index("height")
    own_pixels = pixels // count
    seen = RunningStats()
    for place in list(range(1, count)) + [0]:
        if place == 0:
            own_copy.wait()
        piece = (pieces[place] if place else own_ref)[...]
        start = pl.multiple_of((height ^ place) * own_pixels, own_pixels)
        features_ref[pl.ds(start, own_pixels), :] = piece
        seen.add(piece.astype(wide))
    table_ref[0:1, :], table_ref[1:2, :] = seen.finish(pixels)
    copies[0].wait()
    build_masks(ids_ref, mask_ref, id_rows_ref, id_cols_ref, cols)
    copies[1].wait()
    copies[2].wait()
    table_ref[6:9, :] = gains_ref[...]
    table_ref[9:12, :] = shifts_ref[...]
    for copy in copies[6:]:
        copy.start()
    copies[3].wait()
    copies[4].wait()
    seen = RunningStats()

    def keep(rows, value):
        seen.add(value)
        return value

    run_conv(
        taps_ref,
        product_forward(weights_ref.at[0]),
        mask_ref,
        middle_ref,
        activation(read_input, *norm_rows(table_ref, 0), act_one_ref, taps_ref, cols),
        lambda rows, part: part + biases_ref[0:1, :],
        keep,
        cols,
    )
    table_ref[2:3, :], table_ref[3:4, :] = seen.finish(pixels)
    copies[5].wait()
    seen = RunningStats()
    run_conv(
        taps_ref,
        product_forward(weights_ref.at[1]),
        mask_ref,
        residual_ref,
        activation(read_middle, *norm_rows(table_ref, 1), act_two_ref, taps_ref, cols),
        lambda rows, part: part + (read_input(rows) + biases_ref[1:2, :]),
        keep,
        cols,
    )
    table_ref[4:5, :], table_ref[5:6, :] = seen.finish(pixels)
    for copy in copies[6:]:
        copy.wait()


def score_kernel(
    qv_bias_hbm,
    proj_bias_hbm,
    qkv_ref,
    proj_ref,
    residual_ref,
    table_ref,
    id_rows_ref,
    id_cols_ref,
    normed_ref,
    query_ref,
    key_ref,
    value_ref,
    soft_ref,
    out_flip_ref,
    output_ref,
    qv_bias_ref,
    proj_bias_ref,
    value_flip_ref,
    sems,
    *,
    score_scale,
):
    pixels, channels = residual_ref.shape
    own_pixels = output_ref.shape[0]
    wide = jnp.float32
    exponent = score_scale * 1.4426950408889634
    moves = [(qv_bias_hbm, qv_bias_ref), (proj_bias_hbm, proj_bias_ref)]
    copies = [
        pltpu.make_async_copy(source, target, sems.at[index])
        for index, (source, target) in enumerate(moves)
    ]
    for copy in copies:
        copy.start()
    mean, inverse, gain, shift = norm_rows(table_ref, 2)
    scale = inverse * gain
    for copy in copies:
        copy.wait()
    block = min(QUERY_ROWS, pixels)

    for start in range(0, pixels, block):
        rows = slice(start, start + block)
        normed = ((residual_ref[rows, :] - mean) * scale + shift).astype(jnp.bfloat16)
        normed_ref[rows, :] = normed
        query_ref[rows, :] = (
            jnp.dot(normed, qkv_ref[:, 0:channels], preferred_element_type=wide)
            + qv_bias_ref[0:1, :]
        ).astype(jnp.bfloat16)
        key_ref[rows, :] = jnp.dot(
            normed, qkv_ref[:, channels : 2 * channels], preferred_element_type=wide
        ).astype(jnp.bfloat16)
        values = (
            jnp.dot(normed, qkv_ref[:, 2 * channels :], preferred_element_type=wide)
            + qv_bias_ref[1:2, :]
        ).astype(jnp.bfloat16)
        value_ref[rows, :] = values
        value_flip_ref[:, rows] = values.T
    for start in range(0, pixels, block):
        rows = slice(start, start + block)
        scores = lax.dot_general(
            key_ref[...], query_ref[rows, :], (((1,), (1,)), ((), ())), preferred_element_type=wide
        )
        same = widen(id_rows_ref[...], block) == id_cols_ref[0:1, rows]
        scores = jnp.where(same, scores, masked_score)
        scores = jnp.exp2((scores - jnp.max(scores, axis=0, keepdims=True)) * exponent)
        weights = scores * (1.0 / jnp.sum(scores, axis=0, keepdims=True))
        soft_ref[:, rows] = weights.astype(jnp.bfloat16)
    for start in range(0, pixels, block):
        rows = slice(start, start + block)
        out_flip_ref[:, rows] = jnp.dot(
            value_flip_ref[...], soft_ref[:, rows], preferred_element_type=wide
        ).astype(jnp.bfloat16)
    height = lax.axis_index("height")
    own = pl.ds(pl.multiple_of(height * own_pixels, own_pixels), own_pixels)
    output_ref[...] = (
        residual_ref[own, :]
        + lax.dot_general(
            out_flip_ref[:, own],
            proj_ref[...],
            (((0,), (0,)), ((), ())),
            preferred_element_type=wide,
        )
        + proj_bias_ref[...]
    ).astype(jnp.bfloat16)


def own_quarter():
    height = lax.axis_index("height")
    return (height & 1) * 2 + ((height >> 1) & 1)


def send_order(source_ref, targets, axis, share):
    me = lax.axis_index("canvas")
    for step, target in enumerate(targets):
        place = pl.ds(pl.multiple_of((me ^ step) * share, share), share)
        target[...] = source_ref[place, :] if axis == 0 else source_ref[:, place]


def attention_kernel(
    proj_ref,
    normed_ref,
    query_ref,
    key_ref,
    value_ref,
    soft_ref,
    out_flip_ref,
    *refs,
    score_scale,
    count,
):
    pieces, (grad_ref, packed_ref, sums_ref), refs = (
        refs[:count],
        refs[count : count + 3],
        refs[count + 3 :],
    )
    *mixed_refs, mixed_ref, key_flip_ref, back_ref, score_grad_ref, flip_ref, sems = refs
    pixels, channels = normed_ref.shape
    block = min(QUERY_ROWS, pixels)
    wide = jnp.float32
    copies = place_pieces(pieces, grad_ref, sems)
    for copy in copies:
        copy.start()
    quarter = channels // 4
    own = pl.ds(pl.multiple_of(own_quarter() * quarter, quarter), quarter)
    flip_ref[...] = normed_ref[:, own].T
    key_flip_ref[...] = key_ref[...].T
    for copy in copies:
        copy.wait()
    for start in range(0, pixels, block):
        rows = slice(start, start + block)
        back_ref[rows, :] = lax.dot_general(
            grad_ref[rows, :], proj_ref[...], (((1,), (1,)), ((), ())), preferred_element_type=wide
        ).astype(jnp.bfloat16)
    for start in range(0, pixels, block):
        rows = slice(start, start + block)
        weights = soft_ref[:, rows].astype(wide)
        weight_grad = lax.dot_general(
            value_ref[...],
            back_ref[rows, :],
            (((1,), (1,)), ((), ())),
            preferred_element_type=wide,
        )
        dots = jnp.sum(weights * weight_grad, axis=0, keepdims=True)
        score_grad = (weights * (weight_grad - dots)).astype(jnp.bfloat16)
        score_grad_ref[:, rows] = score_grad
        query_grad = jnp.dot(key_flip_ref[...], score_grad, preferred_element_type=wide)
        packed_ref[rows, 0:channels] = (query_grad * score_scale).astype(jnp.bfloat16).T
        packed_ref[rows, 2 * channels :] = jnp.dot(
            soft_ref[rows, :], back_ref[...], preferred_element_type=wide
        ).astype(jnp.bfloat16)
    for start in range(0, pixels, block):
        rows = slice(start, start + block)
        packed_ref[rows, channels : 2 * channels] = (
            jnp.dot(score_grad_ref[rows, :], query_ref[...], preferred_element_type=wide)
            * score_scale
        ).astype(jnp.bfloat16)

    def pack(rows, carry):
        return (
            carry[0] + fold(packed_ref[rows, 0:channels].astype(wide)),
            carry[1] + fold(packed_ref[rows, 2 * channels :].astype(wide)),
            carry[2] + fold(grad_ref[rows, :].astype(wide)),
        )

    zeros = jnp.zeros((8, channels), wide)
    totals = each_chunk(pixels, pack, (zeros, zeros, zeros))
    sums_ref[...] = jnp.zeros(sums_ref.shape, wide)
    for row, total in enumerate(totals):
        sums_ref[8 + row : 9 + row, :] = column_total(total)
    mixed_ref[:, 0 : 3 * channels] = jnp.dot(
        flip_ref[...], packed_ref[...], preferred_element_type=wide
    ).astype(jnp.bfloat16)
    mixed_ref[:, 3 * channels :] = jnp.dot(
        out_flip_ref[own, :], grad_ref[...], preferred_element_type=wide
    ).astype(jnp.bfloat16)
    send_order(mixed_ref, mixed_refs, 0, quarter // len(mixed_refs))


def third_kernel(
    qkv_ref,
    grad_ref,
    packed_ref,
    residual_ref,
    table_ref,
    act_two_ref,
    mask_ref,
    old_sums_ref,
    residual_grad_ref,
    grad_two_ref,
    sums_ref,
    *refs,
    cols,
):
    *part_refs, total_ref, narrow_ref, columns_ref, part_ref = refs
    pixels, channels = residual_ref.shape
    block = min(CONV_ROWS, pixels)
    wide = jnp.float32
    mean, inverse, gain, shift = norm_rows(table_ref, 2)
    zeros = jnp.zeros((8, channels), wide)

    sums = (zeros, zeros)
    for start in range(0, pixels, block):
        rows = pl.ds(start, block)
        normed_grad = lax.dot_general(
            packed_ref[rows, :], qkv_ref[...], (((1,), (1,)), ((), ())), preferred_element_type=wide
        )
        total_ref[rows, :] = normed_grad
        normed = (residual_ref[rows, :] - mean) * inverse
        sums = sums[0] + fold(normed_grad), sums[1] + fold(normed_grad * normed)
    sums_ref[...] = old_sums_ref[...]
    sums_ref[5:6, :] = column_total(sums[1])
    sums_ref[6:7, :] = column_total(sums[0])
    mean_grad, mean_cross = back_means(sums, gain, pixels)

    def finish(rows, carry):
        normed = (residual_ref[rows, :] - mean) * inverse
        back = inverse * (total_ref[rows, :] * gain - mean_grad - normed * mean_cross)
        total = grad_ref[rows, :].astype(wide) + back
        residual_grad_ref[rows, :] = total
        low = total.astype(jnp.bfloat16)
        grad_two_ref[rows, :] = low
        return carry + fold(low.astype(wide))

    sums_ref[7:8, :] = column_total(each_chunk(pixels, finish, zeros))
    weight_part(act_two_ref, grad_two_ref, mask_ref, narrow_ref, columns_ref, part_ref, cols)
    rows, width = part_refs[0].shape
    send_order(part_ref.at[0:rows, :], part_refs, 1, width)


def second_kernel(
    total_ref,
    partial_ref,
    middle_ref,
    table_ref,
    act_one_ref,
    mask_ref,
    old_sums_ref,
    grad_one_ref,
    sums_ref,
    parts_ref,
    narrow_ref,
    columns_ref,
    part_ref,
    *,
    cols,
):
    pixels, channels = middle_ref.shape
    sums = partial_ref[0:8, :], partial_ref[8:16, :]
    back = norm_back(total_ref, sums, lambda rows: middle_ref[rows, :], table_ref, 1)
    sums_ref[...] = old_sums_ref[...]
    sums_ref[2:3, :] = column_total(sums[1])
    sums_ref[3:4, :] = column_total(sums[0])

    def finish(rows, carry):
        low = back(rows).astype(jnp.bfloat16)
        grad_one_ref[rows, :] = low
        return carry + fold(low.astype(jnp.float32))

    zeros = jnp.zeros((8, channels), jnp.float32)
    sums_ref[4:5, :] = column_total(each_chunk(pixels, finish, zeros))
    weight_part(act_one_ref, grad_one_ref, mask_ref, narrow_ref, columns_ref, part_ref, cols)
    rows, width = parts_ref.shape[1:]
    for piece in range(parts_ref.shape[0]):
        parts_ref[piece] = part_ref[0:rows, piece * width : (piece + 1) * width]


def first_kernel(
    grad_one_ref,
    features_ref,
    residual_grad_ref,
    table_ref,
    mask_ref,
    old_sums_ref,
    weights_ref,
    input_grad_ref,
    sums_ref,
    taps_ref,
    total_ref,
    *,
    cols,
):
    def read(rows):
        return features_ref[rows, :].astype(jnp.float32)

    sums = conv_back(
        grad_one_ref, weights_ref.at[0], mask_ref, taps_ref, total_ref, read, table_ref, 0, cols
    )
    back = norm_back(total_ref, sums, read, table_ref, 0)
    sums_ref[...] = old_sums_ref[...]
    sums_ref[0:1, :] = column_total(sums[1])
    sums_ref[1:2, :] = column_total(sums[0])
    count = input_grad_ref.shape[0]
    own = pl.ds(pl.multiple_of(lax.axis_index("height") * count, count), count)
    input_grad_ref[...] = (residual_grad_ref[own, :] + back(own)).astype(jnp.bfloat16)


def place_kernel(*refs):
    joints, (qkv_hbm, proj_hbm, packed_ref, qkv_ref, proj_ref, sems) = refs[:-6], refs[-6:]
    share = packed_ref.shape[0] // len(joints)
    me = lax.axis_index("canvas")
    for step, joint in enumerate(joints):
        place = pl.ds(pl.multiple_of((me ^ step) * share, share), share)
        packed_ref[place, :] = joint[...]
    spread_quarters([packed_ref], 0, qkv_ref, proj_ref, qkv_hbm, proj_hbm, sems)


def spread_quarters(packed, offset, qkv_ref, proj_ref, qkv_hbm, proj_hbm, sems):
    quarter = packed[0].shape[0]
    inner = qkv_ref.shape[2]
    copies = []
    for index, packed_ref in enumerate(packed):
        owner = own_quarter() ^ (index + offset)
        rows = pl.ds(pl.multiple_of(owner * quarter, quarter), quarter)
        qkv_ref[index] = packed_ref[:, 0:inner].astype(jnp.float32)
        proj_ref[index] = packed_ref[:, inner:].astype(jnp.float32)
        for which, (held, target) in enumerate(((qkv_ref, qkv_hbm), (proj_ref, proj_hbm))):
            copy = pltpu.make_async_copy(held.at[index], target.at[rows, :], sems.at[index, which])
            copy.start()
            copies.append(copy)
    for copy in copies:
        copy.wait()


def join_kernel(*refs):
    ins, (qkv_hbm, proj_hbm, conv_ref, qkv_ref, proj_ref, sems) = refs[:-6], refs[-6:]
    packed, ones_ref, twos = ins[2:5], ins[5], ins[6:]
    ones = [ones_ref[piece] for piece in range(ones_ref.shape[0])]
    twos = [part[...] for part in twos]
    for which, parts in enumerate((ones, twos)):
        total = parts[0].astype(jnp.float32)
        for part in parts[1:]:
            total = total + part.astype(jnp.float32)
        conv_ref[which] = total.reshape(conv_ref.shape[1:])
    spread_quarters(packed, 1, qkv_ref, proj_ref, qkv_hbm, proj_hbm, sems)


def sums_kernel(*refs):
    gains_ref, shifts_ref, conv_ref, qv_ref, proj_ref = refs[-5:]
    total = refs[0][...]
    for ref in refs[1:-5]:
        total = total + ref[...]
    for row, start in enumerate((0, 2, 5)):
        gains_ref[row : row + 1, :] = total[start : start + 1]
        shifts_ref[row : row + 1, :] = total[start + 1 : start + 2]
    conv_ref[0:1, :] = total[4:5]
    conv_ref[1:2, :] = total[7:8]
    qv_ref[...] = total[8:10]
    proj_ref[...] = total[10:11]


def call_kernel(kernel, outputs, scratch, operands, places, flops, limit, out_places=None, aliases={}):
    out_places = out_places or "v" * len(outputs)
    spaces = {
        "v": pl.BlockSpec(memory_space=pltpu.VMEM),
        "s": pl.BlockSpec(memory_space=pltpu.SMEM),
        "h": pl.BlockSpec(memory_space=pl.ANY),
        "o": pl.BlockSpec(memory_space=pltpu.VMEM),
        "a": pl.BlockSpec(memory_space=pl.ANY),
    }
    moved = sum(array.size * array.dtype.itemsize for array in operands)
    held = {"v": pltpu.VMEM, "h": pltpu.HBM, "o": jax.ShapeDtypeStruct}
    operands = [
        pltpu.with_memory_space_constraint(array, pltpu.HBM) if place == "h" else array
        for array, place in zip(operands, places)
    ]
    return pl.pallas_call(
        kernel,
        out_shape=[held[place](*output) for output, place in zip(outputs, out_places)],
        in_specs=[spaces[place] for place in places],
        out_specs=[spaces[place] for place in out_places],
        scratch_shapes=scratch,
        input_output_aliases=aliases,
        compiler_params=pltpu.CompilerParams(vmem_limit_bytes=limit * 2**20),
        cost_estimate=pl.CostEstimate(flops=flops, bytes_accessed=moved, transcendentals=0),
    )(*operands)


def send_height(block, step):
    size = lax.axis_size("height")
    return lax.ppermute(block, "height", [(i, i ^ step) for i in range(size)])


def with_cores(blocks):
    return [piece for block in blocks for piece in (block, send_height(block, 1))]


def trade_canvas(pieces):
    size = lax.axis_size("canvas")
    return [pieces[0]] + [
        lax.ppermute(piece, "canvas", [(i, i ^ step) for i in range(size)])
        for step, piece in enumerate(pieces)
        if step
    ]


def whole_canvas(
    features,
    tile_ids,
    norm_gains,
    norm_shifts,
    conv_weights,
    conv_biases,
    qkv_weight,
    qv_bias,
    proj_weight,
    proj_bias,
    cotangent,
):
    height_size = lax.axis_size("height")
    canvas_size = lax.axis_size("canvas")
    local_rows, cols, channels = features.shape[1:]
    all_rows = tile_ids.shape[1]
    pixels = all_rows * cols
    own_pixels = local_rows * cols
    out_share = channels // height_size
    ci_share = channels // canvas_size
    quarter = channels // 4
    row_share = quarter // canvas_size
    low, wide = jnp.bfloat16, jnp.float32

    own_features = features.reshape(own_pixels, channels)
    own_grad = cotangent.reshape(own_pixels, channels)
    steps = range(2, height_size, 2)
    held_features = [own_features] + [send_height(own_features, step) for step in steps]
    pieces = with_cores(held_features)
    near_grad, pieces[2] = lax.optimization_barrier((own_grad, held_features[1]))
    far_grad, *pieces[4::2] = lax.optimization_barrier((own_grad, *held_features[2:]))
    held_grads = [own_grad, send_height(near_grad, 2)]
    held_grads += [send_height(far_grad, step) for step in steps[1:]]

    part_shape = (9 * out_share, ci_share)
    plane = ((pixels, channels), low)
    plane_wide = ((pixels, channels), wide)
    sums_shape = ((16, channels), wide)
    mixed_shapes = [((row_share, 4 * channels), low)] * canvas_size
    taps = pltpu.VMEM((pixels + 2 * cols, 3 * channels), low)
    held_wide = pltpu.VMEM((pixels, channels), wide)
    flipped = pltpu.VMEM((channels, pixels), low)
    narrow = pltpu.VMEM((pixels + 2 * cols, 3 * NARROW), wide)
    columns = pltpu.VMEM((pixels, 5 * NARROW), low)
    part_held = pltpu.VMEM((5 * NARROW, channels), low)
    sem = pltpu.SemaphoreType.DMA
    conv_flops = 2 * 9 * pixels * channels * channels
    dot_flops = 2 * pixels * channels * channels
    score_flops = 2 * pixels * pixels * channels
    scale = channels ** (-0.5)

    (
        all_features,
        act_one,
        middle,
        act_two,
        residual,
        table,
        mask,
        id_rows,
        id_cols,
        turned,
        held_qkv,
        held_proj,
    ) = call_kernel(
        functools.partial(conv_kernel, cols=cols, count=height_size),
        [
            plane,
            plane,
            plane_wide,
            plane,
            plane_wide,
            ((16, channels), wide),
            ((2, pixels, LANES), wide),
            ((pixels, LANES), jnp.int32),
            ((8, pixels), jnp.int32),
            ((2, 3, channels, 3 * channels), low),
            (qkv_weight.shape, low),
            (proj_weight.shape, low),
        ],
        [
            pltpu.SMEM(tile_ids.shape, jnp.int32),
            pltpu.VMEM(norm_gains.shape, wide),
            pltpu.VMEM(norm_shifts.shape, wide),
            pltpu.VMEM(conv_biases.shape, wide),
            pltpu.VMEM(conv_weights.shape, low),
            taps,
            pltpu.VMEM((own_pixels, channels), low),
            sem((26,)),
            sem,
        ],
        [
            *pieces,
            tile_ids,
            norm_gains,
            norm_shifts,
            conv_biases,
            conv_weights,
            qkv_weight,
            proj_weight,
        ],
        "h" + "v" * (height_size - 1) + "h" * 7,
        2 * conv_flops,
        24,
    )
    residual, *held_grads = lax.optimization_barrier((residual, *held_grads))
    grad_pieces = with_cores(held_grads)
    normed, query, key, value, soft, out_flip, output = call_kernel(
        functools.partial(score_kernel, score_scale=scale),
        [
            plane,
            plane,
            plane,
            plane,
            ((pixels, pixels), low),
            ((channels, pixels), low),
            ((own_pixels, channels), low),
        ],
        [
            pltpu.VMEM(qv_bias.shape, wide),
            pltpu.VMEM((1, channels), wide),
            flipped,
            sem((2,)),
        ],
        [
            qv_bias,
            proj_bias.reshape(1, channels),
            held_qkv,
            held_proj,
            residual,
            table,
            id_rows,
            id_cols,
        ],
        "hhvvvvvv",
        3 * dot_flops + 2 * score_flops,
        16,
        "v" * 6 + "o",
    )
    normed, *grad_pieces = lax.optimization_barrier((normed, *grad_pieces))
    all_grad, packed, sums, *mixed = call_kernel(
        functools.partial(attention_kernel, score_scale=scale, count=height_size),
        [plane, ((pixels, 3 * channels), low), sums_shape, *mixed_shapes],
        [
            pltpu.VMEM((quarter, 4 * channels), low),
            flipped,
            pltpu.VMEM((pixels, channels), low),
            pltpu.VMEM((pixels, pixels), low),
            pltpu.VMEM((quarter, pixels), low),
            sem((height_size,)),
        ],
        [held_proj, normed, query, key, value, soft, out_flip, *grad_pieces],
        "vvvvvvvh" + "a" * (height_size - 1),
        3 * dot_flops + 4 * score_flops,
        20,
    )
    mixed = trade_canvas(mixed)
    residual_grad, grad_two, sums, *parts_two = call_kernel(
        functools.partial(third_kernel, cols=cols),
        [plane_wide, plane, sums_shape] + [(part_shape, low)] * canvas_size,
        [held_wide, narrow, columns, part_held],
        [held_qkv, all_grad, packed, residual, table, act_two, mask, sums],
        "vvvvvvvv",
        3 * dot_flops + conv_flops // height_size,
        16,
    )
    grad_two, *mixed = lax.optimization_barrier((grad_two, *mixed))
    mixed_sum = mixed[0].astype(wide)
    for piece in mixed[1:]:
        mixed_sum = mixed_sum + piece.astype(wide)
    joints = trade_canvas([mixed_sum.astype(low)] * canvas_size)
    act_two_grad, partial_sums = call_kernel(
        functools.partial(turn_kernel, cols=cols),
        [plane_wide, sums_shape],
        [taps],
        [grad_two, mask, turned, middle, table],
        "vvvvv",
        conv_flops,
        16,
    )
    act_two_grad, *joints = lax.optimization_barrier((act_two_grad, *joints))
    qkv_grad, proj_grad, own_mixed = call_kernel(
        place_kernel,
        [(qkv_weight.shape, wide), (proj_weight.shape, wide), ((quarter, 4 * channels), low)],
        [
            pltpu.VMEM((1, quarter, 3 * channels), wide),
            pltpu.VMEM((1, quarter, channels), wide),
            sem((1, 2)),
        ],
        joints,
        "v" * canvas_size,
        0,
        12,
        "hhv",
    )
    chip_mixed = send_height(own_mixed, 2)
    core_mixed = send_height(own_mixed, 1)
    own_mixed, *parts_two = lax.optimization_barrier((own_mixed, *parts_two))
    parts_two = trade_canvas(parts_two)
    grad_one, sums, parts_one = call_kernel(
        functools.partial(second_kernel, cols=cols),
        [plane, sums_shape, ((canvas_size, *part_shape), low)],
        [narrow, columns, part_held],
        [act_two_grad, partial_sums, middle, table, act_one, mask, sums],
        "vvvvvvv",
        conv_flops // height_size,
        16,
    )
    parts_one = lax.all_to_all(parts_one, "canvas", 0, 0)
    input_grad, sums = call_kernel(
        functools.partial(first_kernel, cols=cols),
        [((own_pixels, channels), low), sums_shape],
        [taps, held_wide],
        [grad_one, all_features, residual_grad, table, mask, sums, turned],
        "vvvvvvv",
        conv_flops,
        16,
        "ov",
    )
    sums, chip_mixed, parts_one, *parts_two = lax.optimization_barrier(
        (sums, chip_mixed, parts_one, *parts_two)
    )
    both_mixed = send_height(chip_mixed, 1)
    all_sums = trade_canvas([sums] * canvas_size)
    qkv_grad, proj_grad, conv_grad = call_kernel(
        join_kernel,
        [
            (qkv_weight.shape, wide),
            (proj_weight.shape, wide),
            ((2, 3, 3, out_share, ci_share), wide),
        ],
        [
            pltpu.VMEM((3, quarter, 3 * channels), wide),
            pltpu.VMEM((3, quarter, channels), wide),
            sem((3, 2)),
        ],
        [qkv_grad, proj_grad, chip_mixed, core_mixed, both_mixed, parts_one, *parts_two],
        "hhvvvv" + "v" * canvas_size,
        0,
        12,
        "hho",
        {0: 0, 1: 1},
    )
    conv_grad, *all_sums = lax.optimization_barrier((conv_grad, *all_sums))
    vector_shapes = [norm_gains.shape, norm_shifts.shape, conv_biases.shape, qv_bias.shape]
    gains_grad, shifts_grad, biases_grad, qv_grad, proj_bias_grad = call_kernel(
        sums_kernel,
        [(shape, wide) for shape in vector_shapes + [(1, channels)]],
        [],
        all_sums,
        "v" * canvas_size,
        0,
        16,
        "ooooo",
    )
    own_shape = (1, local_rows, cols, channels)
    return (
        output.reshape(own_shape),
        input_grad.reshape(own_shape),
        gains_grad,
        shifts_grad,
        jnp.swapaxes(conv_grad, 3, 4),
        biases_grad,
        qkv_grad,
        qv_grad,
        proj_grad,
        proj_bias_grad.reshape(channels),
    )


def on_device(*arrays):
    features, tile_ids = arrays[0], arrays[1]
    local_rows, cols, channels = features.shape[1:]
    pixels = tile_ids.shape[1] * cols
    height_size, canvas_size = lax.axis_size("height"), lax.axis_size("canvas")
    powers = all(size & (size - 1) == 0 for size in (height_size, canvas_size, cols))
    fits = (
        powers
        and height_size > 2
        and channels == LANES * canvas_size
        and pixels <= MOST_PIXELS
        and pixels % min(CONV_ROWS, pixels) == 0
        and pixels % FILL_ROWS == 0
        and FILL_ROWS % CHUNK == 0
        and (local_rows * cols) % LANES == 0
        and CHUNK % cols == 0
        and cols % 16 == 0
        and channels % (LANES * canvas_size) == 0
        and 2 * channels == NARROW * height_size
    )
    return whole_canvas(*arrays) if fits else split_canvas(*arrays)


def solution(mesh):
    in_specs = (
        P("canvas", "height", None, None),
        P("canvas", None),
        P(),
        P(),
        P(),
        P(),
        P(),
        P(),
        P(),
        P(),
        P("canvas", "height", None, None),
    )
    out_specs = (
        P("canvas", "height", None, None),
        P("canvas", "height", None, None),
        P(),
        P(),
        P(None, None, None, "canvas", "height"),
        P(),
        P(),
        P(),
        P(),
        P(),
    )
    return jax.shard_map(
        on_device, mesh=mesh, in_specs=in_specs, out_specs=out_specs, check_vma=False
    )
```

```python
import functools

import jax
import jax.numpy as jnp
from jax import lax
from jax.experimental import pallas as pl
from jax.experimental.pallas import tpu as pltpu
from jax.sharding import PartitionSpec as P

GROUPS = 32


epsilon = 1e-06
masked_score = -1e30
MOST_PIXELS = 1024
LANES = 128
NARROW = 128
CHUNK = 128
CONV_ROWS = 1024
FILL_ROWS = 256
QUERY_ROWS = 512


def extended(block, sides, width):
    for axis, dim in sides:
        count = lax.axis_size(axis)
        forward = [(i, i + 1) for i in range(count - 1)]
        backward = [(target, source) for source, target in forward]
        low = lax.ppermute(
            lax.slice_in_dim(block, block.shape[dim] - width, None, axis=dim), axis, forward
        )
        high = lax.ppermute(lax.slice_in_dim(block, 0, width, axis=dim), axis, backward)
        block = jnp.concatenate([low, block, high], axis=dim)
    return block


def group_total(vector):
    return vector.reshape(GROUPS, -1).sum(axis=1)


def spread_groups(vector, channels):
    return jnp.repeat(vector, channels // GROUPS)


def norm_forward(values, gain, shift, members):
    channels = values.shape[1]
    totals = lax.psum(group_total(jnp.sum(values, axis=0)), "height")
    centered = values - spread_groups(totals / members, channels)
    squares = lax.psum(group_total(jnp.sum(centered * centered, axis=0)), "height")
    inverse = spread_groups(lax.rsqrt(squares / members + epsilon), channels)
    normed = centered * inverse
    return (normed, inverse, normed * gain + shift)


def norm_backward(grad_in, normed, inverse, gain, members):
    channels = grad_in.shape[1]
    scaled = grad_in * gain
    both_sums = lax.psum(
        (group_total(jnp.sum(scaled, axis=0)), group_total(jnp.sum(scaled * normed, axis=0))),
        "height",
    )
    mean_grad = spread_groups(both_sums[0] / members, channels)
    mean_cross = spread_groups(both_sums[1] / members, channels)
    result = inverse * (scaled - mean_grad - normed * mean_cross)
    return (result, jnp.sum(grad_in * normed, axis=0), jnp.sum(grad_in, axis=0))


def swish(values):
    return values * jax.nn.sigmoid(values)


def swish_slope(values):
    sigmoid_part = jax.nn.sigmoid(values)
    return sigmoid_part * (1.0 + values * (1.0 - sigmoid_part))


def tap_columns(padded, row_mask, local_rows, canvas_cols):
    pieces = []
    for row_tap in range(3):
        rows_taken = padded[row_tap : row_tap + local_rows] * row_mask[:, row_tap, None, None]
        for col_tap in range(3):
            pieces.append(rows_taken[:, col_tap : col_tap + canvas_cols])
    stacked = jnp.concatenate(pieces, axis=2)
    return stacked.reshape(local_rows * canvas_cols, stacked.shape[2])


def conv_forward(acts, row_mask, weight, bias):
    local_rows, canvas_cols, channels = acts.shape
    rimmed = extended(acts, (("height", 0),), 1)
    padded = jnp.pad(rimmed, ((0, 0), (1, 1), (0, 0)))
    gathered = tap_columns(padded, row_mask, local_rows, canvas_cols)
    result = (
        jnp.dot(
            gathered, weight.reshape(9 * channels, channels), preferred_element_type=jnp.float32
        )
        + bias
    )
    return (result, gathered)


def conv_backward(grad_low, row_mask, weight, gathered):
    local_rows, canvas_cols, channels = grad_low.shape
    flat_grad = grad_low.reshape(local_rows * canvas_cols, channels)
    weight_grad = lax.dot_general(
        gathered, flat_grad, (((0,), (0,)), ((), ())), preferred_element_type=jnp.float32
    )
    rimmed = extended(grad_low, (("height", 0),), 1)
    padded = jnp.pad(rimmed, ((0, 0), (1, 1), (0, 0)))
    grad_taps = tap_columns(padded, row_mask, local_rows, canvas_cols)
    flipped = jnp.transpose(weight[::-1, ::-1], (0, 1, 3, 2)).reshape(9 * channels, channels)
    input_part = jnp.dot(grad_taps, flipped, preferred_element_type=jnp.float32)
    return (
        input_part,
        weight_grad.reshape(3, 3, channels, channels),
        jnp.sum(flat_grad.astype(jnp.float32), axis=0),
    )


def take_rows(array, offset, count):
    return lax.dynamic_slice_in_dim(array, offset, count)


def score_grads(
    queries, out_grad, log_total, row_dots, query_ids, key_rows, value_rows, key_ids, score_scale
):
    scores = (
        lax.dot_general(
            queries, key_rows, (((1,), (1,)), ((), ())), preferred_element_type=jnp.float32
        )
        * score_scale
    )
    same_tile = query_ids[:, None] == key_ids[None, :]
    softmax_block = jnp.exp(jnp.where(same_tile, scores - log_total[:, None], masked_score))
    weight_grad = lax.dot_general(
        out_grad, value_rows, (((1,), (1,)), ((), ())), preferred_element_type=jnp.float32
    )
    score_grad = (softmax_block * (weight_grad - row_dots[:, None])).astype(jnp.bfloat16)
    return (softmax_block.astype(jnp.bfloat16), score_grad)


def split_canvas(
    features,
    tile_ids,
    norm_gains,
    norm_shifts,
    conv_weights,
    conv_biases,
    qkv_weight,
    qv_bias,
    proj_weight,
    proj_bias,
    cotangent,
):
    height_size = lax.axis_size("height")
    local_rows = features.shape[1]
    canvas_cols = features.shape[2]
    channels = features.shape[3]
    pixels = local_rows * canvas_cols
    row_ids = tile_ids[0]
    all_rows = row_ids.shape[0]
    members = float(all_rows * canvas_cols * (channels // GROUPS))
    score_scale = channels ** (-0.5)
    first_row = lax.axis_index("height") * local_rows
    edge_ids = jnp.full((1,), -1, jnp.int32)
    padded_ids = jnp.concatenate([edge_ids, row_ids, edge_ids])
    near_ids = lax.dynamic_slice_in_dim(padded_ids, first_row, local_rows + 2)
    own_rows = near_ids[1 : local_rows + 1]
    row_mask = jnp.stack(
        [near_ids[row_tap : row_tap + local_rows] == own_rows for row_tap in range(3)], axis=1
    ).astype(jnp.bfloat16)
    key_ids = jnp.repeat(row_ids, canvas_cols)
    query_ids = jnp.repeat(own_rows, canvas_cols)
    grid_shape = (local_rows, canvas_cols, channels)
    inputs = features[0].reshape(pixels, channels).astype(jnp.float32)
    normed_one, inverse_one, pre_one = norm_forward(inputs, norm_gains[0], norm_shifts[0], members)
    act_one = swish(pre_one).astype(jnp.bfloat16).reshape(grid_shape)
    middle, taps_one = conv_forward(act_one, row_mask, conv_weights[0], conv_biases[0])
    normed_two, inverse_two, pre_two = norm_forward(middle, norm_gains[1], norm_shifts[1], members)
    act_two = swish(pre_two).astype(jnp.bfloat16).reshape(grid_shape)
    branch, taps_two = conv_forward(act_two, row_mask, conv_weights[1], conv_biases[1])
    residual = inputs + branch
    normed_three, inverse_three, pre_three = norm_forward(
        residual, norm_gains[2], norm_shifts[2], members
    )
    attn_input = pre_three.astype(jnp.bfloat16)
    mixed = jnp.dot(attn_input, qkv_weight, preferred_element_type=jnp.float32)
    queries = (mixed[:, :channels] + qv_bias[0]).astype(jnp.bfloat16)
    key_rows = mixed[:, channels : 2 * channels].astype(jnp.bfloat16)
    value_rows = (mixed[:, 2 * channels :] + qv_bias[1]).astype(jnp.bfloat16)
    running_max = jnp.full((pixels,), masked_score, jnp.float32)
    key_piece = lax.all_gather(key_rows, "height", axis=0, tiled=True)
    value_piece = lax.all_gather(value_rows, "height", axis=0, tiled=True)
    scores = (
        lax.dot_general(
            queries, key_piece, (((1,), (1,)), ((), ())), preferred_element_type=jnp.float32
        )
        * score_scale
    )
    same_tile = query_ids[:, None] == key_ids[None, :]
    scores = jnp.where(same_tile, scores, masked_score)
    new_max = jnp.maximum(running_max, jnp.max(scores, axis=1))
    weights = jnp.where(same_tile, jnp.exp(scores - new_max[:, None]), 0.0)
    summed_out = jnp.dot(
        weights.astype(jnp.bfloat16), value_piece, preferred_element_type=jnp.float32
    )
    total_weight = jnp.sum(weights, axis=1)
    log_total = new_max + jnp.log(total_weight)
    attended = summed_out / total_weight[:, None]
    attended_low = attended.astype(jnp.bfloat16)
    output = (
        residual
        + jnp.dot(attended_low, proj_weight, preferred_element_type=jnp.float32)
        + proj_bias
    )
    out_grad = cotangent[0].reshape(pixels, channels)
    out_grad_full = out_grad.astype(jnp.float32)
    proj_grad = lax.dot_general(
        attended_low, out_grad, (((0,), (0,)), ((), ())), preferred_element_type=jnp.float32
    )
    proj_bias_grad = jnp.sum(out_grad_full, axis=0)
    attended_grad = lax.dot_general(
        out_grad, proj_weight, (((1,), (1,)), ((), ())), preferred_element_type=jnp.float32
    ).astype(jnp.bfloat16)
    row_dots = jnp.sum(attended_grad.astype(jnp.float32) * attended, axis=1)
    block_rows = pixels * min(height_size, 8)
    zero_block = jnp.zeros((pixels, channels), jnp.float32)
    key_all, value_all = (
        lax.all_gather(key_rows, "height", axis=0, tiled=True),
        lax.all_gather(value_rows, "height", axis=0, tiled=True),
    )
    query_all, grad_all = (
        lax.all_gather(queries, "height", axis=0, tiled=True),
        lax.all_gather(attended_grad, "height", axis=0, tiled=True),
    )
    total_all, dots_all = (
        lax.all_gather(log_total, "height", axis=0, tiled=True),
        lax.all_gather(row_dots, "height", axis=0, tiled=True),
    )

    def own_query_step(running, block_index):
        offset = block_index * block_rows
        key_part = take_rows(key_all, offset, block_rows)
        rounded, score_grad = score_grads(
            queries,
            attended_grad,
            log_total,
            row_dots,
            query_ids,
            key_part,
            take_rows(value_all, offset, block_rows),
            take_rows(key_ids, offset, block_rows),
            score_scale,
        )
        return (
            running
            + jnp.dot(score_grad, key_part, preferred_element_type=jnp.float32) * score_scale,
            None,
        )

    def own_key_step(running, block_index):
        offset = block_index * block_rows
        query_part = take_rows(query_all, offset, block_rows)
        grad_part = take_rows(grad_all, offset, block_rows)
        rounded, score_grad = score_grads(
            query_part,
            grad_part,
            take_rows(total_all, offset, block_rows),
            take_rows(dots_all, offset, block_rows),
            take_rows(key_ids, offset, block_rows),
            key_rows,
            value_rows,
            query_ids,
            score_scale,
        )
        key_part = (
            lax.dot_general(
                score_grad, query_part, (((0,), (0,)), ((), ())), preferred_element_type=jnp.float32
            )
            * score_scale
        )
        value_part = lax.dot_general(
            rounded, grad_part, (((0,), (0,)), ((), ())), preferred_element_type=jnp.float32
        )
        return ((running[0] + key_part, running[1] + value_part), None)

    block_count = key_all.shape[0] // block_rows
    query_grad, unused_one = lax.scan(own_query_step, zero_block, jnp.arange(block_count))
    (key_grad, value_grad), unused_two = lax.scan(
        own_key_step, (zero_block, zero_block), jnp.arange(block_count)
    )
    query_low = query_grad.astype(jnp.bfloat16)
    key_low = key_grad.astype(jnp.bfloat16)
    value_low = value_grad.astype(jnp.bfloat16)
    stacked_grad = jnp.concatenate([query_low, key_low, value_low], axis=1)
    qkv_grad = lax.dot_general(
        attn_input, stacked_grad, (((0,), (0,)), ((), ())), preferred_element_type=jnp.float32
    )
    qv_grad = jnp.stack(
        [
            jnp.sum(query_low.astype(jnp.float32), axis=0),
            jnp.sum(value_low.astype(jnp.float32), axis=0),
        ]
    )
    normed_grad = lax.dot_general(
        stacked_grad, qkv_weight, (((1,), (1,)), ((), ())), preferred_element_type=jnp.float32
    )
    back_three, gain_three, shift_three = norm_backward(
        normed_grad, normed_three, inverse_three, norm_gains[2], members
    )
    residual_grad = out_grad_full + back_three
    grad_two = residual_grad.astype(jnp.bfloat16).reshape(grid_shape)
    act_two_grad, weight_two_grad, bias_two_grad = conv_backward(
        grad_two, row_mask, conv_weights[1], taps_two
    )
    middle_grad, gain_two, shift_two = norm_backward(
        act_two_grad * swish_slope(pre_two), normed_two, inverse_two, norm_gains[1], members
    )
    grad_one = middle_grad.astype(jnp.bfloat16).reshape(grid_shape)
    act_one_grad, weight_one_grad, bias_one_grad = conv_backward(
        grad_one, row_mask, conv_weights[0], taps_one
    )
    input_back, gain_one, shift_one = norm_backward(
        act_one_grad * swish_slope(pre_one), normed_one, inverse_one, norm_gains[0], members
    )
    input_grad = residual_grad + input_back
    conv_grad = jnp.stack([weight_one_grad, weight_two_grad])
    conv_part = lax.psum_scatter(conv_grad, "height", scatter_dimension=4, tiled=True)
    conv_part = lax.psum_scatter(
        conv_part.astype(jnp.bfloat16), "canvas", scatter_dimension=3, tiled=True
    ).astype(jnp.float32)
    summed = lax.psum(
        (
            jnp.stack([gain_one, gain_two, gain_three]),
            jnp.stack([shift_one, shift_two, shift_three]),
            jnp.stack([bias_one_grad, bias_two_grad]),
            qkv_grad,
            qv_grad,
            proj_grad,
            proj_bias_grad,
        ),
        ("canvas", "height"),
    )
    return (
        output.astype(jnp.bfloat16).reshape((1,) + grid_shape),
        input_grad.astype(jnp.bfloat16).reshape((1,) + grid_shape),
        summed[0],
        summed[1],
        conv_part,
        summed[2],
        summed[3],
        summed[4],
        summed[5],
        summed[6],
    )


def fold(block):
    rows, width = block.shape
    return jnp.sum(block.reshape(rows // 8, 8, width), axis=0)


def group_lanes(block, group):
    lane = lax.broadcasted_iota(jnp.int32, block.shape, 1)
    width = block.shape[1]
    step = 1
    while step < group:
        above = pltpu.roll(block, step, 1)
        below = pltpu.roll(block, width - step, 1)
        block = block + jnp.where((lane & step) != 0, above, below)
        step *= 2
    return block


def group_mean(partial, members):
    spread = group_lanes(partial, partial.shape[1] // GROUPS)
    return jnp.sum(spread, axis=0, keepdims=True) * (1.0 / members)


def widen(block, width):
    return jnp.concatenate([block] * (width // block.shape[1]), axis=1)


def each_block(pixels, block, body, carry=0):
    def step(index, carry):
        return body(pl.ds(pl.multiple_of(index * block, block), block), carry)

    return lax.fori_loop(0, pixels // block, step, carry)


def each_chunk(pixels, body, carry):
    return each_block(pixels, CHUNK, body, carry)


def aligned(start, step):
    return start if isinstance(start, int) else pl.multiple_of(start, step)


def fold_about(block, center):
    rows, width = block.shape
    offset = block.reshape(rows // 8, 8, width) - center[None]
    return jnp.sum(offset, axis=0), jnp.sum(offset * offset, axis=0)


def finish_stats(center, sums, squares, pixels):
    width = center.shape[1] // GROUPS
    share = pixels / 8.0
    means = center + sums * (1.0 / share)
    spread = squares - sums * sums * (1.0 / share)
    mean = group_mean(means, 8.0 * width)
    offset = means - mean
    variance = group_mean(spread + share * offset * offset, float(pixels * width))
    return mean, lax.rsqrt(variance + epsilon)


class RunningStats:
    def __init__(self):
        self.center = None

    def add(self, block):
        if self.center is None:
            self.center = block[0:8]
            self.sums, self.squares = fold_about(block, self.center)
        else:
            sums, squares = fold_about(block, self.center)
            self.sums, self.squares = self.sums + sums, self.squares + squares

    def finish(self, pixels):
        return finish_stats(self.center, self.sums, self.squares, pixels)


def put_taps(taps_ref, block, rows, cols):
    count, channels = block.shape
    place = lax.broadcasted_iota(jnp.int32, block.shape, 0) & (cols - 1)
    left = jnp.where(place == 0, 0.0, pltpu.roll(block, 1, 0))
    right = jnp.where(place == cols - 1, 0.0, pltpu.roll(block, count - 1, 0))
    inner = pl.ds(aligned(rows.start + cols, cols), count)
    taps_ref[inner, 0:channels] = left.astype(jnp.bfloat16)
    taps_ref[inner, channels : 2 * channels] = block.astype(jnp.bfloat16)
    taps_ref[inner, 2 * channels :] = right.astype(jnp.bfloat16)


def clear_edges(taps_ref, cols):
    edge = jnp.zeros((cols, taps_ref.shape[1]), taps_ref.dtype)
    taps_ref[0:cols, :] = edge
    taps_ref[taps_ref.shape[0] - cols :, :] = edge


def run_conv(taps_ref, product, mask_ref, total_ref, fill, first, last, cols):
    pixels, channels = total_ref.shape
    for start in range(0, pixels, FILL_ROWS):
        for inner in range(start, start + FILL_ROWS, CHUNK):
            fill(pl.ds(inner, CHUNK))
        rows = pl.ds(start, FILL_ROWS)
        total_ref[rows, :] = first(rows, product(taps_ref, pl.ds(start + cols, FILL_ROWS), 1))
    block = min(CONV_ROWS, pixels)
    for row_tap in (0, 2):
        for start in range(0, pixels, block):
            rows = pl.ds(start, block)
            part = product(taps_ref, pl.ds(start + row_tap * cols, block), row_tap)
            mask = widen(mask_ref[row_tap // 2, rows, :], channels)
            value = total_ref[rows, :] + mask * part
            total_ref[rows, :] = value if row_tap == 0 else last(rows, value)


def product_forward(weight_ref):
    channels = weight_ref.shape[-1]

    def product(taps_ref, shifted, row_tap):
        return jnp.dot(
            taps_ref[shifted, :],
            weight_ref[row_tap].reshape(3 * channels, channels),
            preferred_element_type=jnp.float32,
        )

    return product


def product_backward(weight_ref):
    def product(taps_ref, shifted, row_tap):
        return lax.dot_general(
            taps_ref[shifted, :],
            weight_ref[row_tap],
            (((1,), (1,)), ((), ())),
            preferred_element_type=jnp.float32,
        )

    return product


def smooth(values):
    part = 0.5 * jnp.tanh(0.5 * values) + 0.5
    return values * part, part


def activation(read, mean, inverse, gain, shift, act_ref, taps_ref, cols):
    scale = inverse * gain

    def fill(rows):
        act = smooth((read(rows) - mean) * scale + shift)[0]
        act_ref[rows, :] = act.astype(jnp.bfloat16)
        put_taps(taps_ref, act, rows, cols)

    return fill


def back_means(sums, gain, pixels):
    channels = gain.shape[1]
    members = float(pixels * (channels // GROUPS))
    return group_mean(sums[0] * gain, members), group_mean(sums[1] * gain, members)


def column_total(partial):
    return jnp.sum(partial, axis=0, keepdims=True)


def weight_part(act_ref, grad_ref, mask_ref, narrow_ref, columns_ref, part_ref, cols):
    pixels, channels = act_ref.shape
    height = lax.axis_index("height")
    share = NARROW // 2
    block = pl.ds(pl.multiple_of((height // 2) * NARROW, NARROW), NARROW)
    parity = height % 2
    edge = jnp.zeros((cols, 3 * NARROW), jnp.float32)
    narrow_ref[0:cols, :] = edge
    narrow_ref[cols + pixels :, :] = edge

    def spread(rows, carry):
        own = grad_ref[rows, block].astype(jnp.float32)
        half = lax.broadcasted_iota(jnp.int32, own.shape, 1) // share
        turned = pltpu.roll(own, share, 1)
        both = jnp.where(half == parity, own, turned)
        place = lax.broadcasted_iota(jnp.int32, own.shape, 0) & (cols - 1)
        left = jnp.where(place == 0, 0.0, pltpu.roll(both, 1, 0))
        right = jnp.where(place == cols - 1, 0.0, pltpu.roll(both, CHUNK - 1, 0))
        inner = pl.ds(aligned(rows.start + cols, cols), CHUNK)
        narrow_ref[inner, 0:NARROW] = left
        narrow_ref[inner, NARROW : 2 * NARROW] = both
        narrow_ref[inner, 2 * NARROW :] = right
        return carry

    each_chunk(pixels, spread, 0)

    def gather(rows, carry):
        taps = []
        for row_tap in range(3):
            for col_tap in range(3):
                row_back, col_back = 2 - row_tap, 2 - col_tap
                shifted = pl.ds(aligned(rows.start + row_back * cols, cols), CHUNK)
                block = narrow_ref[shifted, col_back * NARROW : (col_back + 1) * NARROW]
                if row_back != 1:
                    block = block * mask_ref[row_back // 2, rows, :]
                taps.append(block)
        lower = lax.broadcasted_iota(jnp.int32, taps[0].shape, 1) < share
        for pair in range(5):
            second = taps[min(2 * pair + 1, 8)]
            columns_ref[rows, pair * NARROW : (pair + 1) * NARROW] = jnp.where(
                lower, taps[2 * pair], second
            ).astype(jnp.bfloat16)
        return carry

    each_chunk(pixels, gather, 0)
    part_ref[...] = lax.dot_general(
        columns_ref[...],
        act_ref[...],
        (((0,), (0,)), ((), ())),
        preferred_element_type=jnp.float32,
    ).astype(jnp.bfloat16)


def conv_back(grad_ref, weights_ref, mask_ref, taps_ref, total_ref, read, table_ref, which, cols):
    clear_edges(taps_ref, cols)
    mean, inverse, gain, shift = norm_rows(table_ref, which)
    sums = []

    def fill(rows):
        put_taps(taps_ref, grad_ref[rows, :].astype(jnp.float32), rows, cols)

    def slope(rows, value):
        normed = (read(rows) - mean) * inverse
        pre = normed * gain + shift
        part = smooth(pre)[1]
        grad = value * (part * (1.0 + pre * (1.0 - part)))
        sums.append((fold(grad), fold(grad * normed)))
        return grad

    run_conv(
        taps_ref,
        product_backward(weights_ref),
        mask_ref,
        total_ref,
        fill,
        lambda rows, part: part,
        slope,
        cols,
    )
    return sum(pair[0] for pair in sums), sum(pair[1] for pair in sums)


def norm_back(total_ref, sums, read, table_ref, which):
    mean, inverse, gain, shift = norm_rows(table_ref, which)
    mean_grad, mean_cross = back_means(sums, gain, total_ref.shape[0])

    def back(rows):
        normed = (read(rows) - mean) * inverse
        return inverse * (total_ref[rows, :] * gain - mean_grad - normed * mean_cross)

    return back


def turn_kernel(
    grad_ref, mask_ref, weights_ref, middle_ref, table_ref, total_ref, sums_ref, taps_ref, *, cols
):
    sums_ref[0:8, :], sums_ref[8:16, :] = conv_back(
        grad_ref,
        weights_ref.at[1],
        mask_ref,
        taps_ref,
        total_ref,
        lambda rows: middle_ref[rows, :],
        table_ref,
        1,
        cols,
    )


def norm_rows(table_ref, which):
    picks = (2 * which, 2 * which + 1, 6 + which, 9 + which)
    return tuple(table_ref[pick : pick + 1, :] for pick in picks)


def build_masks(ids_ref, mask_ref, id_rows_ref, id_cols_ref, cols):
    rows = ids_ref.shape[1]
    for row in range(rows):
        here = ids_ref[0, row]
        place = slice(row * cols, (row + 1) * cols)
        id_rows_ref[place, :] = jnp.full((cols, LANES), here, jnp.int32)
        for side, other in ((0, row - 1), (1, row + 1)):
            same = jnp.float32(0.0)
            if 0 <= other < rows:
                same = jnp.where(ids_ref[0, other] == here, 1.0, 0.0).astype(jnp.float32)
            mask_ref[side, place, :] = jnp.full((cols, LANES), same, jnp.float32)
    lane = lax.broadcasted_iota(jnp.int32, (8, LANES), 1)
    each = LANES // cols
    for block in range(rows // each):
        ids = jnp.full((8, LANES), ids_ref[0, block * each], jnp.int32)
        for step in range(1, each):
            ids = jnp.where(lane >= step * cols, ids_ref[0, block * each + step], ids)
        id_cols_ref[:, block * LANES : (block + 1) * LANES] = ids


def place_pieces(pieces, whole_ref, sems):
    own_pixels = whole_ref.shape[0] // len(pieces)
    height = lax.axis_index("height")
    copies = []
    for place, piece in enumerate(pieces):
        start = pl.multiple_of((height ^ place) * own_pixels, own_pixels)
        rows = pl.ds(start, own_pixels)
        copies.append(pltpu.make_async_copy(piece, whole_ref.at[rows, :], sems.at[place]))
    return copies


def conv_kernel(*refs, cols, count):
    pieces, refs = refs[:count], refs[count:]
    (
        ids_hbm,
        gains_hbm,
        shifts_hbm,
        biases_hbm,
        weights_hbm,
        qkv_hbm,
        proj_hbm,
        features_ref,
        act_one_ref,
        middle_ref,
        act_two_ref,
        residual_ref,
        table_ref,
        mask_ref,
        id_rows_ref,
        id_cols_ref,
        turned_ref,
        qkv_ref,
        proj_ref,
        ids_ref,
        gains_ref,
        shifts_ref,
        biases_ref,
        weights_ref,
        taps_ref,
        own_ref,
        sems,
        piece_sem,
    ) = refs
    pixels, channels = features_ref.shape
    wide = jnp.float32
    turned = [
        (
            weights_hbm.at[which, 2 - row_tap, 2 - col_tap],
            turned_ref.at[which, row_tap, :, col_tap * channels : (col_tap + 1) * channels],
        )
        for which in (1, 0)
        for row_tap in range(3)
        for col_tap in range(3)
    ]
    moves = [
        (ids_hbm, ids_ref),
        (gains_hbm, gains_ref),
        (shifts_hbm, shifts_ref),
        (weights_hbm.at[0], weights_ref.at[0]),
        (biases_hbm, biases_ref),
        (weights_hbm.at[1], weights_ref.at[1]),
        (qkv_hbm, qkv_ref),
        (proj_hbm, proj_ref),
    ] + turned
    copies = [
        pltpu.make_async_copy(source, target, sems.at[index])
        for index, (source, target) in enumerate(moves)
    ]
    own_copy = pltpu.make_async_copy(pieces[0], own_ref, piece_sem)
    for copy in [own_copy] + copies[:6]:
        copy.start()
    clear_edges(taps_ref, cols)

    def read_input(rows):
        return features_ref[rows, :].astype(wide)

    def read_middle(rows):
        return middle_ref[rows, :]

    height = lax.axis_index("height")
    own_pixels = pixels // count
    seen = RunningStats()
    for place in list(range(1, count)) + [0]:
        if place == 0:
            own_copy.wait()
        piece = (pieces[place] if place else own_ref)[...]
        start = pl.multiple_of((height ^ place) * own_pixels, own_pixels)
        features_ref[pl.ds(start, own_pixels), :] = piece
        seen.add(piece.astype(wide))
    table_ref[0:1, :], table_ref[1:2, :] = seen.finish(pixels)
    copies[0].wait()
    build_masks(ids_ref, mask_ref, id_rows_ref, id_cols_ref, cols)
    copies[1].wait()
    copies[2].wait()
    table_ref[6:9, :] = gains_ref[...]
    table_ref[9:12, :] = shifts_ref[...]
    for copy in copies[6:]:
        copy.start()
    copies[3].wait()
    copies[4].wait()
    seen = RunningStats()

    def keep(rows, value):
        seen.add(value)
        return value

    run_conv(
        taps_ref,
        product_forward(weights_ref.at[0]),
        mask_ref,
        middle_ref,
        activation(read_input, *norm_rows(table_ref, 0), act_one_ref, taps_ref, cols),
        lambda rows, part: part + biases_ref[0:1, :],
        keep,
        cols,
    )
    table_ref[2:3, :], table_ref[3:4, :] = seen.finish(pixels)
    copies[5].wait()
    seen = RunningStats()
    run_conv(
        taps_ref,
        product_forward(weights_ref.at[1]),
        mask_ref,
        residual_ref,
        activation(read_middle, *norm_rows(table_ref, 1), act_two_ref, taps_ref, cols),
        lambda rows, part: part + (read_input(rows) + biases_ref[1:2, :]),
        keep,
        cols,
    )
    table_ref[4:5, :], table_ref[5:6, :] = seen.finish(pixels)
    for copy in copies[6:]:
        copy.wait()


def score_kernel(
    qv_bias_hbm,
    proj_bias_hbm,
    qkv_ref,
    proj_ref,
    residual_ref,
    table_ref,
    id_rows_ref,
    id_cols_ref,
    normed_ref,
    query_ref,
    key_ref,
    value_ref,
    soft_ref,
    out_flip_ref,
    output_ref,
    qv_bias_ref,
    proj_bias_ref,
    value_flip_ref,
    sems,
    *,
    score_scale,
):
    pixels, channels = residual_ref.shape
    own_pixels = output_ref.shape[0]
    wide = jnp.float32
    exponent = score_scale * 1.4426950408889634
    moves = [(qv_bias_hbm, qv_bias_ref), (proj_bias_hbm, proj_bias_ref)]
    copies = [
        pltpu.make_async_copy(source, target, sems.at[index])
        for index, (source, target) in enumerate(moves)
    ]
    for copy in copies:
        copy.start()
    mean, inverse, gain, shift = norm_rows(table_ref, 2)
    scale = inverse * gain
    for copy in copies:
        copy.wait()
    block = min(QUERY_ROWS, pixels)

    def project(index, carry):
        rows = pl.ds(pl.multiple_of(index * block, block), block)
        normed = ((residual_ref[rows, :] - mean) * scale + shift).astype(jnp.bfloat16)
        normed_ref[rows, :] = normed
        query_ref[rows, :] = (
            jnp.dot(normed, qkv_ref[:, 0:channels], preferred_element_type=wide)
            + qv_bias_ref[0:1, :]
        ).astype(jnp.bfloat16)
        key_ref[rows, :] = jnp.dot(
            normed, qkv_ref[:, channels : 2 * channels], preferred_element_type=wide
        ).astype(jnp.bfloat16)
        values = (
            jnp.dot(normed, qkv_ref[:, 2 * channels :], preferred_element_type=wide)
            + qv_bias_ref[1:2, :]
        ).astype(jnp.bfloat16)
        value_ref[rows, :] = values
        value_flip_ref[:, rows] = values.T
        return carry

    lax.fori_loop(0, pixels // block, project, 0)

    def attend(index, carry):
        rows = pl.ds(pl.multiple_of(index * block, block), block)
        scores = lax.dot_general(
            key_ref[...], query_ref[rows, :], (((1,), (1,)), ((), ())), preferred_element_type=wide
        )
        same = widen(id_rows_ref[...], block) == id_cols_ref[0:1, rows]
        scores = jnp.where(same, scores, masked_score)
        scores = jnp.exp2((scores - jnp.max(scores, axis=0, keepdims=True)) * exponent)
        weights = scores * (1.0 / jnp.sum(scores, axis=0, keepdims=True))
        rounded = weights.astype(jnp.bfloat16)
        soft_ref[:, rows] = rounded
        out_flip_ref[:, rows] = jnp.dot(
            value_flip_ref[...], rounded, preferred_element_type=wide
        ).astype(jnp.bfloat16)
        return carry

    lax.fori_loop(0, pixels // block, attend, 0)
    height = lax.axis_index("height")
    own = pl.ds(pl.multiple_of(height * own_pixels, own_pixels), own_pixels)
    output_ref[...] = (
        residual_ref[own, :]
        + lax.dot_general(
            out_flip_ref[:, own],
            proj_ref[...],
            (((0,), (0,)), ((), ())),
            preferred_element_type=wide,
        )
        + proj_bias_ref[...]
    ).astype(jnp.bfloat16)


def own_quarter():
    height = lax.axis_index("height")
    return (height & 1) * 2 + ((height >> 1) & 1)


def send_order(source_ref, targets, axis, share):
    me = lax.axis_index("canvas")
    for step, target in enumerate(targets):
        place = pl.ds(pl.multiple_of((me ^ step) * share, share), share)
        target[...] = source_ref[place, :] if axis == 0 else source_ref[:, place]


def attention_kernel(
    proj_ref,
    normed_ref,
    query_ref,
    key_ref,
    value_ref,
    soft_ref,
    out_flip_ref,
    *refs,
    score_scale,
    count,
):
    pieces, (grad_ref, packed_ref, sums_ref), refs = (
        refs[:count],
        refs[count : count + 3],
        refs[count + 3 :],
    )
    *mixed_refs, mixed_ref, key_flip_ref, back_ref, score_grad_ref, flip_ref, sems = refs
    pixels, channels = normed_ref.shape
    block = min(QUERY_ROWS, pixels)
    wide = jnp.float32
    copies = place_pieces(pieces, grad_ref, sems)
    for copy in copies:
        copy.start()
    quarter = channels // 4
    own = pl.ds(pl.multiple_of(own_quarter() * quarter, quarter), quarter)
    flip_ref[...] = normed_ref[:, own].T
    key_flip_ref[...] = key_ref[...].T
    for copy in copies:
        copy.wait()

    def project(rows, carry):
        back_ref[rows, :] = lax.dot_general(
            grad_ref[rows, :], proj_ref[...], (((1,), (1,)), ((), ())), preferred_element_type=wide
        ).astype(jnp.bfloat16)
        return carry

    def soften(rows, carry):
        weights = soft_ref[:, rows].astype(wide)
        weight_grad = lax.dot_general(
            value_ref[...],
            back_ref[rows, :],
            (((1,), (1,)), ((), ())),
            preferred_element_type=wide,
        )
        dots = jnp.sum(weights * weight_grad, axis=0, keepdims=True)
        score_grad = (weights * (weight_grad - dots)).astype(jnp.bfloat16)
        score_grad_ref[:, rows] = score_grad
        query_grad = jnp.dot(key_flip_ref[...], score_grad, preferred_element_type=wide)
        packed_ref[rows, 0:channels] = (query_grad * score_scale).astype(jnp.bfloat16).T
        return carry

    def collect(rows, carry):
        packed_ref[rows, channels : 2 * channels] = (
            jnp.dot(score_grad_ref[rows, :], query_ref[...], preferred_element_type=wide)
            * score_scale
        ).astype(jnp.bfloat16)
        packed_ref[rows, 2 * channels :] = jnp.dot(
            soft_ref[rows, :], back_ref[...], preferred_element_type=wide
        ).astype(jnp.bfloat16)
        return carry

    each_block(pixels, block, project)
    each_block(pixels, block, soften)
    each_block(pixels, block, collect)

    def pack(rows, carry):
        return (
            carry[0] + fold(packed_ref[rows, 0:channels].astype(wide)),
            carry[1] + fold(packed_ref[rows, 2 * channels :].astype(wide)),
            carry[2] + fold(grad_ref[rows, :].astype(wide)),
        )

    zeros = jnp.zeros((8, channels), wide)
    totals = each_chunk(pixels, pack, (zeros, zeros, zeros))
    sums_ref[...] = jnp.zeros(sums_ref.shape, wide)
    for row, total in enumerate(totals):
        sums_ref[8 + row : 9 + row, :] = column_total(total)
    mixed_ref[:, 0 : 3 * channels] = jnp.dot(
        flip_ref[...], packed_ref[...], preferred_element_type=wide
    ).astype(jnp.bfloat16)
    mixed_ref[:, 3 * channels :] = jnp.dot(
        out_flip_ref[own, :], grad_ref[...], preferred_element_type=wide
    ).astype(jnp.bfloat16)
    send_order(mixed_ref, mixed_refs, 0, quarter // len(mixed_refs))


def third_kernel(
    qkv_ref,
    grad_ref,
    packed_ref,
    residual_ref,
    table_ref,
    act_two_ref,
    mask_ref,
    old_sums_ref,
    residual_grad_ref,
    grad_two_ref,
    sums_ref,
    part_ref,
    total_ref,
    narrow_ref,
    columns_ref,
    *,
    cols,
):
    pixels, channels = residual_ref.shape
    block = min(CONV_ROWS, pixels)
    wide = jnp.float32
    mean, inverse, gain, shift = norm_rows(table_ref, 2)
    zeros = jnp.zeros((8, channels), wide)

    sums = (zeros, zeros)
    for start in range(0, pixels, block):
        rows = pl.ds(start, block)
        normed_grad = lax.dot_general(
            packed_ref[rows, :], qkv_ref[...], (((1,), (1,)), ((), ())), preferred_element_type=wide
        )
        total_ref[rows, :] = normed_grad
        normed = (residual_ref[rows, :] - mean) * inverse
        sums = sums[0] + fold(normed_grad), sums[1] + fold(normed_grad * normed)
    sums_ref[...] = old_sums_ref[...]
    sums_ref[5:6, :] = column_total(sums[1])
    sums_ref[6:7, :] = column_total(sums[0])
    mean_grad, mean_cross = back_means(sums, gain, pixels)

    def finish(rows, carry):
        normed = (residual_ref[rows, :] - mean) * inverse
        back = inverse * (total_ref[rows, :] * gain - mean_grad - normed * mean_cross)
        total = grad_ref[rows, :].astype(wide) + back
        residual_grad_ref[rows, :] = total
        low = total.astype(jnp.bfloat16)
        grad_two_ref[rows, :] = low
        return carry + fold(low.astype(wide))

    sums_ref[7:8, :] = column_total(each_chunk(pixels, finish, zeros))
    weight_part(act_two_ref, grad_two_ref, mask_ref, narrow_ref, columns_ref, part_ref, cols)


def second_kernel(
    total_ref,
    partial_ref,
    middle_ref,
    table_ref,
    act_one_ref,
    mask_ref,
    old_sums_ref,
    part_two_ref,
    grad_one_ref,
    sums_ref,
    *refs,
    cols,
):
    *both_refs, narrow_ref, columns_ref, part_ref = refs
    pixels, channels = middle_ref.shape
    sums = partial_ref[0:8, :], partial_ref[8:16, :]
    back = norm_back(total_ref, sums, lambda rows: middle_ref[rows, :], table_ref, 1)
    sums_ref[...] = old_sums_ref[...]
    sums_ref[2:3, :] = column_total(sums[1])
    sums_ref[3:4, :] = column_total(sums[0])

    def finish(rows, carry):
        low = back(rows).astype(jnp.bfloat16)
        grad_one_ref[rows, :] = low
        return carry + fold(low.astype(jnp.float32))

    zeros = jnp.zeros((8, channels), jnp.float32)
    sums_ref[4:5, :] = column_total(each_chunk(pixels, finish, zeros))
    weight_part(act_one_ref, grad_one_ref, mask_ref, narrow_ref, columns_ref, part_ref, cols)
    rows, width = both_refs[0].shape
    for which, source_ref in enumerate((part_ref, part_two_ref)):
        place = slice(which * rows // 2, (which + 1) * rows // 2)
        targets = [both_ref.at[place, :] for both_ref in both_refs]
        send_order(source_ref.at[0 : rows // 2, :], targets, 1, width)


def first_kernel(
    grad_one_ref,
    features_ref,
    residual_grad_ref,
    table_ref,
    mask_ref,
    old_sums_ref,
    weights_ref,
    input_grad_ref,
    sums_ref,
    taps_ref,
    total_ref,
    *,
    cols,
):
    def read(rows):
        return features_ref[rows, :].astype(jnp.float32)

    sums = conv_back(
        grad_one_ref, weights_ref.at[0], mask_ref, taps_ref, total_ref, read, table_ref, 0, cols
    )
    back = norm_back(total_ref, sums, read, table_ref, 0)
    sums_ref[...] = old_sums_ref[...]
    sums_ref[0:1, :] = column_total(sums[1])
    sums_ref[1:2, :] = column_total(sums[0])
    count = input_grad_ref.shape[0]
    own = pl.ds(pl.multiple_of(lax.axis_index("height") * count, count), count)
    input_grad_ref[...] = (residual_grad_ref[own, :] + back(own)).astype(jnp.bfloat16)


def place_kernel(*refs):
    joints, (qkv_hbm, proj_hbm, packed_ref, qkv_ref, proj_ref, sems) = refs[:-6], refs[-6:]
    share = packed_ref.shape[0] // len(joints)
    me = lax.axis_index("canvas")
    for step, joint in enumerate(joints):
        place = pl.ds(pl.multiple_of((me ^ step) * share, share), share)
        packed_ref[place, :] = joint[...]
    spread_quarters([packed_ref], 0, qkv_ref, proj_ref, qkv_hbm, proj_hbm, sems)


def spread_quarters(packed, offset, qkv_ref, proj_ref, qkv_hbm, proj_hbm, sems):
    quarter = packed[0].shape[0]
    inner = qkv_ref.shape[2]
    copies = []
    for index, packed_ref in enumerate(packed):
        owner = own_quarter() ^ (index + offset)
        rows = pl.ds(pl.multiple_of(owner * quarter, quarter), quarter)
        qkv_ref[index] = packed_ref[:, 0:inner].astype(jnp.float32)
        proj_ref[index] = packed_ref[:, inner:].astype(jnp.float32)
        for which, (held, target) in enumerate(((qkv_ref, qkv_hbm), (proj_ref, proj_hbm))):
            copy = pltpu.make_async_copy(held.at[index], target.at[rows, :], sems.at[index, which])
            copy.start()
            copies.append(copy)
    for copy in copies:
        copy.wait()


def join_kernel(*refs):
    ins, (qkv_hbm, proj_hbm, qkv_ref, proj_ref, sems) = refs[:-5], refs[-5:]
    packed = ins[2:]
    spread_quarters(packed, 1, qkv_ref, proj_ref, qkv_hbm, proj_hbm, sems)


def sums_kernel(*refs):
    parts, (share_ref, gains_ref, shifts_ref, conv_ref, qv_ref, proj_ref) = refs[2:-6], refs[-6:]
    total = refs[0][...] + refs[1][...]
    for row, start in enumerate((0, 2, 5)):
        gains_ref[row : row + 1, :] = total[start : start + 1]
        shifts_ref[row : row + 1, :] = total[start + 1 : start + 2]
    conv_ref[0:1, :] = total[4:5]
    conv_ref[1:2, :] = total[7:8]
    qv_ref[...] = total[8:10]
    proj_ref[...] = total[10:11]
    shares = parts[0][...].astype(jnp.float32)
    for part in parts[1:]:
        shares = shares + part[...].astype(jnp.float32)
    share_ref[...] = shares.reshape(share_ref.shape)


def call_kernel(kernel, outputs, scratch, operands, places, flops, limit, out_places=None, aliases={}):
    out_places = out_places or "v" * len(outputs)
    spaces = {
        "v": pl.BlockSpec(memory_space=pltpu.VMEM),
        "s": pl.BlockSpec(memory_space=pltpu.SMEM),
        "h": pl.BlockSpec(memory_space=pl.ANY),
        "o": pl.BlockSpec(memory_space=pltpu.VMEM),
        "a": pl.BlockSpec(memory_space=pl.ANY),
    }
    moved = sum(array.size * array.dtype.itemsize for array in operands)
    held = {"v": pltpu.VMEM, "h": pltpu.HBM, "o": jax.ShapeDtypeStruct}
    operands = [
        pltpu.with_memory_space_constraint(array, pltpu.HBM) if place == "h" else array
        for array, place in zip(operands, places)
    ]
    return pl.pallas_call(
        kernel,
        out_shape=[held[place](*output) for output, place in zip(outputs, out_places)],
        in_specs=[spaces[place] for place in places],
        out_specs=[spaces[place] for place in out_places],
        scratch_shapes=scratch,
        input_output_aliases=aliases,
        compiler_params=pltpu.CompilerParams(vmem_limit_bytes=limit * 2**20),
        cost_estimate=pl.CostEstimate(flops=flops, bytes_accessed=moved, transcendentals=0),
    )(*operands)


def send_height(block, step):
    size = lax.axis_size("height")
    return lax.ppermute(block, "height", [(i, i ^ step) for i in range(size)])


def with_cores(blocks):
    return [piece for block in blocks for piece in (block, send_height(block, 1))]


def trade_canvas(pieces):
    size = lax.axis_size("canvas")
    return [pieces[0]] + [
        lax.ppermute(piece, "canvas", [(i, i ^ step) for i in range(size)])
        for step, piece in enumerate(pieces)
        if step
    ]


def whole_canvas(
    features,
    tile_ids,
    norm_gains,
    norm_shifts,
    conv_weights,
    conv_biases,
    qkv_weight,
    qv_bias,
    proj_weight,
    proj_bias,
    cotangent,
):
    height_size = lax.axis_size("height")
    canvas_size = lax.axis_size("canvas")
    local_rows, cols, channels = features.shape[1:]
    all_rows = tile_ids.shape[1]
    pixels = all_rows * cols
    own_pixels = local_rows * cols
    out_share = channels // height_size
    ci_share = channels // canvas_size
    quarter = channels // 4
    row_share = quarter // canvas_size
    low, wide = jnp.bfloat16, jnp.float32

    own_features = features.reshape(own_pixels, channels)
    own_grad = cotangent.reshape(own_pixels, channels)
    steps = range(2, height_size, 2)
    held_features = [own_features] + [send_height(own_features, step) for step in steps]
    pieces = with_cores(held_features)
    near_grad, pieces[2] = lax.optimization_barrier((own_grad, held_features[1]))
    far_grad, *pieces[4::2] = lax.optimization_barrier((own_grad, *held_features[2:]))
    held_grads = [own_grad, send_height(near_grad, 2)]
    held_grads += [send_height(far_grad, step) for step in steps[1:]]

    plane = ((pixels, channels), low)
    plane_wide = ((pixels, channels), wide)
    sums_shape = ((16, channels), wide)
    mixed_shapes = [((row_share, 4 * channels), low)] * canvas_size
    taps = pltpu.VMEM((pixels + 2 * cols, 3 * channels), low)
    held_wide = pltpu.VMEM((pixels, channels), wide)
    flipped = pltpu.VMEM((channels, pixels), low)
    narrow = pltpu.VMEM((pixels + 2 * cols, 3 * NARROW), wide)
    columns = pltpu.VMEM((pixels, 5 * NARROW), low)
    part_held = pltpu.VMEM((5 * NARROW, channels), low)
    sem = pltpu.SemaphoreType.DMA
    conv_flops = 2 * 9 * pixels * channels * channels
    dot_flops = 2 * pixels * channels * channels
    score_flops = 2 * pixels * pixels * channels
    scale = channels ** (-0.5)

    (
        all_features,
        act_one,
        middle,
        act_two,
        residual,
        table,
        mask,
        id_rows,
        id_cols,
        turned,
        held_qkv,
        held_proj,
    ) = call_kernel(
        functools.partial(conv_kernel, cols=cols, count=height_size),
        [
            plane,
            plane,
            plane_wide,
            plane,
            plane_wide,
            ((16, channels), wide),
            ((2, pixels, LANES), wide),
            ((pixels, LANES), jnp.int32),
            ((8, pixels), jnp.int32),
            ((2, 3, channels, 3 * channels), low),
            (qkv_weight.shape, low),
            (proj_weight.shape, low),
        ],
        [
            pltpu.SMEM(tile_ids.shape, jnp.int32),
            pltpu.VMEM(norm_gains.shape, wide),
            pltpu.VMEM(norm_shifts.shape, wide),
            pltpu.VMEM(conv_biases.shape, wide),
            pltpu.VMEM(conv_weights.shape, low),
            taps,
            pltpu.VMEM((own_pixels, channels), low),
            sem((26,)),
            sem,
        ],
        [
            *pieces,
            tile_ids,
            norm_gains,
            norm_shifts,
            conv_biases,
            conv_weights,
            qkv_weight,
            proj_weight,
        ],
        "h" + "v" * (height_size - 1) + "h" * 7,
        2 * conv_flops,
        24,
    )
    residual, *held_grads = lax.optimization_barrier((residual, *held_grads))
    grad_pieces = with_cores(held_grads)
    normed, query, key, value, soft, out_flip, output = call_kernel(
        functools.partial(score_kernel, score_scale=scale),
        [
            plane,
            plane,
            plane,
            plane,
            ((pixels, pixels), low),
            ((channels, pixels), low),
            ((own_pixels, channels), low),
        ],
        [
            pltpu.VMEM(qv_bias.shape, wide),
            pltpu.VMEM((1, channels), wide),
            flipped,
            sem((2,)),
        ],
        [
            qv_bias,
            proj_bias.reshape(1, channels),
            held_qkv,
            held_proj,
            residual,
            table,
            id_rows,
            id_cols,
        ],
        "hhvvvvvv",
        3 * dot_flops + 2 * score_flops,
        16,
        "v" * 6 + "o",
    )
    normed, *grad_pieces = lax.optimization_barrier((normed, *grad_pieces))
    all_grad, packed, sums, *mixed = call_kernel(
        functools.partial(attention_kernel, score_scale=scale, count=height_size),
        [plane, ((pixels, 3 * channels), low), sums_shape, *mixed_shapes],
        [
            pltpu.VMEM((quarter, 4 * channels), low),
            flipped,
            pltpu.VMEM((pixels, channels), low),
            pltpu.VMEM((pixels, pixels), low),
            pltpu.VMEM((quarter, pixels), low),
            sem((height_size,)),
        ],
        [held_proj, normed, query, key, value, soft, out_flip, *grad_pieces],
        "vvvvvvvh" + "a" * (height_size - 1),
        3 * dot_flops + 4 * score_flops,
        20,
    )
    mixed = trade_canvas(mixed)
    residual_grad, grad_two, sums, part_two = call_kernel(
        functools.partial(third_kernel, cols=cols),
        [plane_wide, plane, sums_shape, ((5 * NARROW, channels), low)],
        [held_wide, narrow, columns],
        [held_qkv, all_grad, packed, residual, table, act_two, mask, sums],
        "vvvvvvvv",
        3 * dot_flops + conv_flops // height_size,
        16,
    )
    grad_two, *mixed = lax.optimization_barrier((grad_two, *mixed))
    mixed_sum = mixed[0].astype(wide)
    for piece in mixed[1:]:
        mixed_sum = mixed_sum + piece.astype(wide)
    joints = trade_canvas([mixed_sum.astype(low)] * canvas_size)
    act_two_grad, partial_sums = call_kernel(
        functools.partial(turn_kernel, cols=cols),
        [plane_wide, sums_shape],
        [taps],
        [grad_two, mask, turned, middle, table],
        "vvvvv",
        conv_flops,
        16,
    )
    act_two_grad, *joints = lax.optimization_barrier((act_two_grad, *joints))
    qkv_grad, proj_grad, own_mixed = call_kernel(
        place_kernel,
        [(qkv_weight.shape, wide), (proj_weight.shape, wide), ((quarter, 4 * channels), low)],
        [
            pltpu.VMEM((1, quarter, 3 * channels), wide),
            pltpu.VMEM((1, quarter, channels), wide),
            sem((1, 2)),
        ],
        joints,
        "v" * canvas_size,
        0,
        12,
        "hhv",
    )
    chip_mixed = send_height(own_mixed, 2)
    core_mixed = send_height(own_mixed, 1)
    grad_one, sums, *both_parts = call_kernel(
        functools.partial(second_kernel, cols=cols),
        [plane, sums_shape] + [((18 * out_share, ci_share), low)] * canvas_size,
        [narrow, columns, part_held],
        [act_two_grad, partial_sums, middle, table, act_one, mask, sums, part_two],
        "vvvvvvvv",
        conv_flops // height_size,
        16,
    )
    both_parts = trade_canvas(both_parts)
    input_grad, sums = call_kernel(
        functools.partial(first_kernel, cols=cols),
        [((own_pixels, channels), low), sums_shape],
        [taps, held_wide],
        [grad_one, all_features, residual_grad, table, mask, sums, turned],
        "vvvvvvv",
        conv_flops,
        16,
        "ov",
    )
    sums, chip_mixed, core_mixed, *both_parts[1:-1] = lax.optimization_barrier(
        (sums, chip_mixed, core_mixed, *both_parts[1:-1])
    )
    both_mixed = send_height(chip_mixed, 1)
    step = 1
    while step < canvas_size:
        last_sums = sums, lax.ppermute(
            sums, "canvas", [(i, i ^ step) for i in range(canvas_size)]
        )
        step *= 2
        if step < canvas_size:
            sums = last_sums[0] + last_sums[1]
    qkv_grad, proj_grad = call_kernel(
        join_kernel,
        [(qkv_weight.shape, wide), (proj_weight.shape, wide)],
        [
            pltpu.VMEM((3, quarter, 3 * channels), wide),
            pltpu.VMEM((3, quarter, channels), wide),
            sem((3, 2)),
        ],
        [qkv_grad, proj_grad, chip_mixed, core_mixed, both_mixed],
        "hhvvv",
        0,
        12,
        "hh",
        {0: 0, 1: 1},
    )
    qkv_grad, last, both_parts[-1] = lax.optimization_barrier(
        (qkv_grad, last_sums[1], both_parts[-1])
    )
    last_sums = last_sums[0], last
    vector_shapes = [norm_gains.shape, norm_shifts.shape, conv_biases.shape, qv_bias.shape]
    conv_grad, gains_grad, shifts_grad, biases_grad, qv_grad, proj_bias_grad = call_kernel(
        sums_kernel,
        [((2, 3, 3, out_share, ci_share), wide)]
        + [(shape, wide) for shape in vector_shapes + [(1, channels)]],
        [],
        [*last_sums, *both_parts],
        "vv" + "v" * canvas_size,
        0,
        12,
        "o" * 6,
    )
    own_shape = (1, local_rows, cols, channels)
    return (
        output.reshape(own_shape),
        input_grad.reshape(own_shape),
        gains_grad,
        shifts_grad,
        jnp.swapaxes(conv_grad, 3, 4),
        biases_grad,
        qkv_grad,
        qv_grad,
        proj_grad,
        proj_bias_grad.reshape(channels),
    )


def on_device(*arrays):
    features, tile_ids = arrays[0], arrays[1]
    local_rows, cols, channels = features.shape[1:]
    pixels = tile_ids.shape[1] * cols
    height_size, canvas_size = lax.axis_size("height"), lax.axis_size("canvas")
    powers = all(size & (size - 1) == 0 for size in (height_size, canvas_size, cols))
    fits = (
        powers
        and height_size > 2
        and canvas_size > 1
        and channels == LANES * canvas_size
        and pixels <= MOST_PIXELS
        and pixels % min(CONV_ROWS, pixels) == 0
        and pixels % FILL_ROWS == 0
        and FILL_ROWS % CHUNK == 0
        and (local_rows * cols) % LANES == 0
        and CHUNK % cols == 0
        and cols % 16 == 0
        and channels % (LANES * canvas_size) == 0
        and 2 * channels == NARROW * height_size
    )
    return whole_canvas(*arrays) if fits else split_canvas(*arrays)


def solution(mesh):
    in_specs = (
        P("canvas", "height", None, None),
        P("canvas", None),
        P(),
        P(),
        P(),
        P(),
        P(),
        P(),
        P(),
        P(),
        P("canvas", "height", None, None),
    )
    out_specs = (
        P("canvas", "height", None, None),
        P("canvas", "height", None, None),
        P(),
        P(),
        P(None, None, None, "canvas", "height"),
        P(),
        P(),
        P(),
        P(),
        P(),
    )
    return jax.shard_map(
        on_device, mesh=mesh, in_specs=in_specs, out_specs=out_specs, check_vma=False
    )
```

```python
import functools

import jax
import jax.numpy as jnp
from jax import lax
from jax.experimental import pallas as pl
from jax.experimental.pallas import tpu as pltpu
from jax.sharding import PartitionSpec as P

GROUPS = 32


epsilon = 1e-06
masked_score = -1e30
MOST_PIXELS = 1024
LANES = 128
NARROW = 128
CHUNK = 128
CONV_ROWS = 1024
FILL_ROWS = 256
QUERY_ROWS = 512


def extended(block, sides, width):
    for axis, dim in sides:
        count = lax.axis_size(axis)
        forward = [(i, i + 1) for i in range(count - 1)]
        backward = [(target, source) for source, target in forward]
        low = lax.ppermute(
            lax.slice_in_dim(block, block.shape[dim] - width, None, axis=dim), axis, forward
        )
        high = lax.ppermute(lax.slice_in_dim(block, 0, width, axis=dim), axis, backward)
        block = jnp.concatenate([low, block, high], axis=dim)
    return block


def group_total(vector):
    return vector.reshape(GROUPS, -1).sum(axis=1)


def spread_groups(vector, channels):
    return jnp.repeat(vector, channels // GROUPS)


def norm_forward(values, gain, shift, members):
    channels = values.shape[1]
    totals = lax.psum(group_total(jnp.sum(values, axis=0)), "height")
    centered = values - spread_groups(totals / members, channels)
    squares = lax.psum(group_total(jnp.sum(centered * centered, axis=0)), "height")
    inverse = spread_groups(lax.rsqrt(squares / members + epsilon), channels)
    normed = centered * inverse
    return (normed, inverse, normed * gain + shift)


def norm_backward(grad_in, normed, inverse, gain, members):
    channels = grad_in.shape[1]
    scaled = grad_in * gain
    both_sums = lax.psum(
        (group_total(jnp.sum(scaled, axis=0)), group_total(jnp.sum(scaled * normed, axis=0))),
        "height",
    )
    mean_grad = spread_groups(both_sums[0] / members, channels)
    mean_cross = spread_groups(both_sums[1] / members, channels)
    result = inverse * (scaled - mean_grad - normed * mean_cross)
    return (result, jnp.sum(grad_in * normed, axis=0), jnp.sum(grad_in, axis=0))


def swish(values):
    return values * jax.nn.sigmoid(values)


def swish_slope(values):
    sigmoid_part = jax.nn.sigmoid(values)
    return sigmoid_part * (1.0 + values * (1.0 - sigmoid_part))


def tap_columns(padded, row_mask, local_rows, canvas_cols):
    pieces = []
    for row_tap in range(3):
        rows_taken = padded[row_tap : row_tap + local_rows] * row_mask[:, row_tap, None, None]
        for col_tap in range(3):
            pieces.append(rows_taken[:, col_tap : col_tap + canvas_cols])
    stacked = jnp.concatenate(pieces, axis=2)
    return stacked.reshape(local_rows * canvas_cols, stacked.shape[2])


def conv_forward(acts, row_mask, weight, bias):
    local_rows, canvas_cols, channels = acts.shape
    rimmed = extended(acts, (("height", 0),), 1)
    padded = jnp.pad(rimmed, ((0, 0), (1, 1), (0, 0)))
    gathered = tap_columns(padded, row_mask, local_rows, canvas_cols)
    result = (
        jnp.dot(
            gathered, weight.reshape(9 * channels, channels), preferred_element_type=jnp.float32
        )
        + bias
    )
    return (result, gathered)


def conv_backward(grad_low, row_mask, weight, gathered):
    local_rows, canvas_cols, channels = grad_low.shape
    flat_grad = grad_low.reshape(local_rows * canvas_cols, channels)
    weight_grad = lax.dot_general(
        gathered, flat_grad, (((0,), (0,)), ((), ())), preferred_element_type=jnp.float32
    )
    rimmed = extended(grad_low, (("height", 0),), 1)
    padded = jnp.pad(rimmed, ((0, 0), (1, 1), (0, 0)))
    grad_taps = tap_columns(padded, row_mask, local_rows, canvas_cols)
    flipped = jnp.transpose(weight[::-1, ::-1], (0, 1, 3, 2)).reshape(9 * channels, channels)
    input_part = jnp.dot(grad_taps, flipped, preferred_element_type=jnp.float32)
    return (
        input_part,
        weight_grad.reshape(3, 3, channels, channels),
        jnp.sum(flat_grad.astype(jnp.float32), axis=0),
    )


def take_rows(array, offset, count):
    return lax.dynamic_slice_in_dim(array, offset, count)


def score_grads(
    queries, out_grad, log_total, row_dots, query_ids, key_rows, value_rows, key_ids, score_scale
):
    scores = (
        lax.dot_general(
            queries, key_rows, (((1,), (1,)), ((), ())), preferred_element_type=jnp.float32
        )
        * score_scale
    )
    same_tile = query_ids[:, None] == key_ids[None, :]
    softmax_block = jnp.exp(jnp.where(same_tile, scores - log_total[:, None], masked_score))
    weight_grad = lax.dot_general(
        out_grad, value_rows, (((1,), (1,)), ((), ())), preferred_element_type=jnp.float32
    )
    score_grad = (softmax_block * (weight_grad - row_dots[:, None])).astype(jnp.bfloat16)
    return (softmax_block.astype(jnp.bfloat16), score_grad)


def split_canvas(
    features,
    tile_ids,
    norm_gains,
    norm_shifts,
    conv_weights,
    conv_biases,
    qkv_weight,
    qv_bias,
    proj_weight,
    proj_bias,
    cotangent,
):
    height_size = lax.axis_size("height")
    local_rows = features.shape[1]
    canvas_cols = features.shape[2]
    channels = features.shape[3]
    pixels = local_rows * canvas_cols
    row_ids = tile_ids[0]
    all_rows = row_ids.shape[0]
    members = float(all_rows * canvas_cols * (channels // GROUPS))
    score_scale = channels ** (-0.5)
    first_row = lax.axis_index("height") * local_rows
    edge_ids = jnp.full((1,), -1, jnp.int32)
    padded_ids = jnp.concatenate([edge_ids, row_ids, edge_ids])
    near_ids = lax.dynamic_slice_in_dim(padded_ids, first_row, local_rows + 2)
    own_rows = near_ids[1 : local_rows + 1]
    row_mask = jnp.stack(
        [near_ids[row_tap : row_tap + local_rows] == own_rows for row_tap in range(3)], axis=1
    ).astype(jnp.bfloat16)
    key_ids = jnp.repeat(row_ids, canvas_cols)
    query_ids = jnp.repeat(own_rows, canvas_cols)
    grid_shape = (local_rows, canvas_cols, channels)
    inputs = features[0].reshape(pixels, channels).astype(jnp.float32)
    normed_one, inverse_one, pre_one = norm_forward(inputs, norm_gains[0], norm_shifts[0], members)
    act_one = swish(pre_one).astype(jnp.bfloat16).reshape(grid_shape)
    middle, taps_one = conv_forward(act_one, row_mask, conv_weights[0], conv_biases[0])
    normed_two, inverse_two, pre_two = norm_forward(middle, norm_gains[1], norm_shifts[1], members)
    act_two = swish(pre_two).astype(jnp.bfloat16).reshape(grid_shape)
    branch, taps_two = conv_forward(act_two, row_mask, conv_weights[1], conv_biases[1])
    residual = inputs + branch
    normed_three, inverse_three, pre_three = norm_forward(
        residual, norm_gains[2], norm_shifts[2], members
    )
    attn_input = pre_three.astype(jnp.bfloat16)
    mixed = jnp.dot(attn_input, qkv_weight, preferred_element_type=jnp.float32)
    queries = (mixed[:, :channels] + qv_bias[0]).astype(jnp.bfloat16)
    key_rows = mixed[:, channels : 2 * channels].astype(jnp.bfloat16)
    value_rows = (mixed[:, 2 * channels :] + qv_bias[1]).astype(jnp.bfloat16)
    running_max = jnp.full((pixels,), masked_score, jnp.float32)
    key_piece = lax.all_gather(key_rows, "height", axis=0, tiled=True)
    value_piece = lax.all_gather(value_rows, "height", axis=0, tiled=True)
    scores = (
        lax.dot_general(
            queries, key_piece, (((1,), (1,)), ((), ())), preferred_element_type=jnp.float32
        )
        * score_scale
    )
    same_tile = query_ids[:, None] == key_ids[None, :]
    scores = jnp.where(same_tile, scores, masked_score)
    new_max = jnp.maximum(running_max, jnp.max(scores, axis=1))
    weights = jnp.where(same_tile, jnp.exp(scores - new_max[:, None]), 0.0)
    summed_out = jnp.dot(
        weights.astype(jnp.bfloat16), value_piece, preferred_element_type=jnp.float32
    )
    total_weight = jnp.sum(weights, axis=1)
    log_total = new_max + jnp.log(total_weight)
    attended = summed_out / total_weight[:, None]
    attended_low = attended.astype(jnp.bfloat16)
    output = (
        residual
        + jnp.dot(attended_low, proj_weight, preferred_element_type=jnp.float32)
        + proj_bias
    )
    out_grad = cotangent[0].reshape(pixels, channels)
    out_grad_full = out_grad.astype(jnp.float32)
    proj_grad = lax.dot_general(
        attended_low, out_grad, (((0,), (0,)), ((), ())), preferred_element_type=jnp.float32
    )
    proj_bias_grad = jnp.sum(out_grad_full, axis=0)
    attended_grad = lax.dot_general(
        out_grad, proj_weight, (((1,), (1,)), ((), ())), preferred_element_type=jnp.float32
    ).astype(jnp.bfloat16)
    row_dots = jnp.sum(attended_grad.astype(jnp.float32) * attended, axis=1)
    block_rows = pixels * min(height_size, 8)
    zero_block = jnp.zeros((pixels, channels), jnp.float32)
    key_all, value_all = (
        lax.all_gather(key_rows, "height", axis=0, tiled=True),
        lax.all_gather(value_rows, "height", axis=0, tiled=True),
    )
    query_all, grad_all = (
        lax.all_gather(queries, "height", axis=0, tiled=True),
        lax.all_gather(attended_grad, "height", axis=0, tiled=True),
    )
    total_all, dots_all = (
        lax.all_gather(log_total, "height", axis=0, tiled=True),
        lax.all_gather(row_dots, "height", axis=0, tiled=True),
    )

    def own_query_step(running, block_index):
        offset = block_index * block_rows
        key_part = take_rows(key_all, offset, block_rows)
        rounded, score_grad = score_grads(
            queries,
            attended_grad,
            log_total,
            row_dots,
            query_ids,
            key_part,
            take_rows(value_all, offset, block_rows),
            take_rows(key_ids, offset, block_rows),
            score_scale,
        )
        return (
            running
            + jnp.dot(score_grad, key_part, preferred_element_type=jnp.float32) * score_scale,
            None,
        )

    def own_key_step(running, block_index):
        offset = block_index * block_rows
        query_part = take_rows(query_all, offset, block_rows)
        grad_part = take_rows(grad_all, offset, block_rows)
        rounded, score_grad = score_grads(
            query_part,
            grad_part,
            take_rows(total_all, offset, block_rows),
            take_rows(dots_all, offset, block_rows),
            take_rows(key_ids, offset, block_rows),
            key_rows,
            value_rows,
            query_ids,
            score_scale,
        )
        key_part = (
            lax.dot_general(
                score_grad, query_part, (((0,), (0,)), ((), ())), preferred_element_type=jnp.float32
            )
            * score_scale
        )
        value_part = lax.dot_general(
            rounded, grad_part, (((0,), (0,)), ((), ())), preferred_element_type=jnp.float32
        )
        return ((running[0] + key_part, running[1] + value_part), None)

    block_count = key_all.shape[0] // block_rows
    query_grad, unused_one = lax.scan(own_query_step, zero_block, jnp.arange(block_count))
    (key_grad, value_grad), unused_two = lax.scan(
        own_key_step, (zero_block, zero_block), jnp.arange(block_count)
    )
    query_low = query_grad.astype(jnp.bfloat16)
    key_low = key_grad.astype(jnp.bfloat16)
    value_low = value_grad.astype(jnp.bfloat16)
    stacked_grad = jnp.concatenate([query_low, key_low, value_low], axis=1)
    qkv_grad = lax.dot_general(
        attn_input, stacked_grad, (((0,), (0,)), ((), ())), preferred_element_type=jnp.float32
    )
    qv_grad = jnp.stack(
        [
            jnp.sum(query_low.astype(jnp.float32), axis=0),
            jnp.sum(value_low.astype(jnp.float32), axis=0),
        ]
    )
    normed_grad = lax.dot_general(
        stacked_grad, qkv_weight, (((1,), (1,)), ((), ())), preferred_element_type=jnp.float32
    )
    back_three, gain_three, shift_three = norm_backward(
        normed_grad, normed_three, inverse_three, norm_gains[2], members
    )
    residual_grad = out_grad_full + back_three
    grad_two = residual_grad.astype(jnp.bfloat16).reshape(grid_shape)
    act_two_grad, weight_two_grad, bias_two_grad = conv_backward(
        grad_two, row_mask, conv_weights[1], taps_two
    )
    middle_grad, gain_two, shift_two = norm_backward(
        act_two_grad * swish_slope(pre_two), normed_two, inverse_two, norm_gains[1], members
    )
    grad_one = middle_grad.astype(jnp.bfloat16).reshape(grid_shape)
    act_one_grad, weight_one_grad, bias_one_grad = conv_backward(
        grad_one, row_mask, conv_weights[0], taps_one
    )
    input_back, gain_one, shift_one = norm_backward(
        act_one_grad * swish_slope(pre_one), normed_one, inverse_one, norm_gains[0], members
    )
    input_grad = residual_grad + input_back
    conv_grad = jnp.stack([weight_one_grad, weight_two_grad])
    conv_part = lax.psum_scatter(conv_grad, "height", scatter_dimension=4, tiled=True)
    conv_part = lax.psum_scatter(
        conv_part.astype(jnp.bfloat16), "canvas", scatter_dimension=3, tiled=True
    ).astype(jnp.float32)
    summed = lax.psum(
        (
            jnp.stack([gain_one, gain_two, gain_three]),
            jnp.stack([shift_one, shift_two, shift_three]),
            jnp.stack([bias_one_grad, bias_two_grad]),
            qkv_grad,
            qv_grad,
            proj_grad,
            proj_bias_grad,
        ),
        ("canvas", "height"),
    )
    return (
        output.astype(jnp.bfloat16).reshape((1,) + grid_shape),
        input_grad.astype(jnp.bfloat16).reshape((1,) + grid_shape),
        summed[0],
        summed[1],
        conv_part,
        summed[2],
        summed[3],
        summed[4],
        summed[5],
        summed[6],
    )


def fold(block):
    rows, width = block.shape
    return jnp.sum(block.reshape(rows // 8, 8, width), axis=0)


def group_lanes(block, group):
    lane = lax.broadcasted_iota(jnp.int32, block.shape, 1)
    width = block.shape[1]
    step = 1
    while step < group:
        above = pltpu.roll(block, step, 1)
        below = pltpu.roll(block, width - step, 1)
        block = block + jnp.where((lane & step) != 0, above, below)
        step *= 2
    return block


def group_mean(partial, members):
    spread = group_lanes(partial, partial.shape[1] // GROUPS)
    return jnp.sum(spread, axis=0, keepdims=True) * (1.0 / members)


def widen(block, width):
    return jnp.concatenate([block] * (width // block.shape[1]), axis=1)


def each_block(pixels, block, body, carry=0):
    def step(index, carry):
        return body(pl.ds(pl.multiple_of(index * block, block), block), carry)

    return lax.fori_loop(0, pixels // block, step, carry)


def each_chunk(pixels, body, carry):
    return each_block(pixels, CHUNK, body, carry)


def aligned(start, step):
    return start if isinstance(start, int) else pl.multiple_of(start, step)


def fold_about(block, center):
    rows, width = block.shape
    offset = block.reshape(rows // 8, 8, width) - center[None]
    return jnp.sum(offset, axis=0), jnp.sum(offset * offset, axis=0)


def finish_stats(center, sums, squares, pixels):
    width = center.shape[1] // GROUPS
    share = pixels / 8.0
    means = center + sums * (1.0 / share)
    spread = squares - sums * sums * (1.0 / share)
    mean = group_mean(means, 8.0 * width)
    offset = means - mean
    variance = group_mean(spread + share * offset * offset, float(pixels * width))
    return mean, lax.rsqrt(variance + epsilon)


class RunningStats:
    def __init__(self):
        self.center = None

    def add(self, block):
        if self.center is None:
            self.center = block[0:8]
            self.sums, self.squares = fold_about(block, self.center)
        else:
            sums, squares = fold_about(block, self.center)
            self.sums, self.squares = self.sums + sums, self.squares + squares

    def finish(self, pixels):
        return finish_stats(self.center, self.sums, self.squares, pixels)


def put_taps(taps_ref, block, rows, cols):
    count, channels = block.shape
    place = lax.broadcasted_iota(jnp.int32, block.shape, 0) & (cols - 1)
    left = jnp.where(place == 0, 0.0, pltpu.roll(block, 1, 0))
    right = jnp.where(place == cols - 1, 0.0, pltpu.roll(block, count - 1, 0))
    inner = pl.ds(aligned(rows.start + cols, cols), count)
    taps_ref[inner, 0:channels] = left.astype(jnp.bfloat16)
    taps_ref[inner, channels : 2 * channels] = block.astype(jnp.bfloat16)
    taps_ref[inner, 2 * channels :] = right.astype(jnp.bfloat16)


def clear_edges(taps_ref, cols):
    edge = jnp.zeros((cols, taps_ref.shape[1]), taps_ref.dtype)
    taps_ref[0:cols, :] = edge
    taps_ref[taps_ref.shape[0] - cols :, :] = edge


def run_conv(taps_ref, product, mask_ref, total_ref, fill, first, last, cols):
    pixels, channels = total_ref.shape
    for start in range(0, pixels, FILL_ROWS):
        for inner in range(start, start + FILL_ROWS, CHUNK):
            fill(pl.ds(inner, CHUNK))
        rows = pl.ds(start, FILL_ROWS)
        total_ref[rows, :] = first(rows, product(taps_ref, pl.ds(start + cols, FILL_ROWS), 1))
    block = min(CONV_ROWS, pixels)
    for row_tap in (0, 2):
        for start in range(0, pixels, block):
            rows = pl.ds(start, block)
            part = product(taps_ref, pl.ds(start + row_tap * cols, block), row_tap)
            mask = widen(mask_ref[row_tap // 2, rows, :], channels)
            value = total_ref[rows, :] + mask * part
            total_ref[rows, :] = value if row_tap == 0 else last(rows, value)


def product_forward(weight_ref):
    channels = weight_ref.shape[-1]

    def product(taps_ref, shifted, row_tap):
        return jnp.dot(
            taps_ref[shifted, :],
            weight_ref[row_tap].reshape(3 * channels, channels),
            preferred_element_type=jnp.float32,
        )

    return product


def product_backward(weight_ref):
    def product(taps_ref, shifted, row_tap):
        return lax.dot_general(
            taps_ref[shifted, :],
            weight_ref[row_tap],
            (((1,), (1,)), ((), ())),
            preferred_element_type=jnp.float32,
        )

    return product


def smooth(values):
    part = 0.5 * jnp.tanh(0.5 * values) + 0.5
    return values * part, part


def activation(read, mean, inverse, gain, shift, act_ref, taps_ref, cols):
    scale = inverse * gain

    def fill(rows):
        act = smooth((read(rows) - mean) * scale + shift)[0]
        act_ref[rows, :] = act.astype(jnp.bfloat16)
        put_taps(taps_ref, act, rows, cols)

    return fill


def back_means(sums, gain, pixels):
    channels = gain.shape[1]
    members = float(pixels * (channels // GROUPS))
    return group_mean(sums[0] * gain, members), group_mean(sums[1] * gain, members)


def column_total(partial):
    return jnp.sum(partial, axis=0, keepdims=True)


def weight_part(act_ref, grad_ref, lanes_ref, flip_ref, columns_ref, part_ref, cols):
    pixels, channels = act_ref.shape
    height = lax.axis_index("height")
    share = NARROW // 2
    block = pl.ds(pl.multiple_of((height // 2) * NARROW, NARROW), NARROW)
    flip_ref[...] = grad_ref[:, block].T
    own = pl.ds(pl.multiple_of((height % 2) * share, share), share)
    grad = flip_ref[own, :].astype(jnp.float32)
    place = lax.broadcasted_iota(jnp.int32, grad.shape, 1) & (cols - 1)
    for col_tap in range(3):
        shifted = grad
        if col_tap == 0:
            shifted = jnp.where(place == cols - 1, 0.0, pltpu.roll(grad, pixels - 1, 1))
        elif col_tap == 2:
            shifted = jnp.where(place == 0, 0.0, pltpu.roll(grad, 1, 1))
        for row_tap in range(3):
            moved = shifted
            if row_tap == 0:
                moved = pltpu.roll(shifted, pixels - cols, 1) * lanes_ref[1:2, :]
            elif row_tap == 2:
                moved = pltpu.roll(shifted, cols, 1) * lanes_ref[0:1, :]
            tap = 3 * row_tap + col_tap
            columns_ref[tap * share : (tap + 1) * share, :] = moved.astype(jnp.bfloat16)
    part_ref[...] = jnp.dot(
        columns_ref[...], act_ref[...], preferred_element_type=jnp.float32
    ).astype(jnp.bfloat16)


def conv_back(grad_ref, weights_ref, mask_ref, taps_ref, total_ref, read, table_ref, which, cols):
    clear_edges(taps_ref, cols)
    mean, inverse, gain, shift = norm_rows(table_ref, which)
    sums = []

    def fill(rows):
        put_taps(taps_ref, grad_ref[rows, :].astype(jnp.float32), rows, cols)

    def slope(rows, value):
        normed = (read(rows) - mean) * inverse
        pre = normed * gain + shift
        part = smooth(pre)[1]
        grad = value * (part * (1.0 + pre * (1.0 - part)))
        sums.append((fold(grad), fold(grad * normed)))
        return grad

    run_conv(
        taps_ref,
        product_backward(weights_ref),
        mask_ref,
        total_ref,
        fill,
        lambda rows, part: part,
        slope,
        cols,
    )
    return sum(pair[0] for pair in sums), sum(pair[1] for pair in sums)


def norm_back(total_ref, sums, read, table_ref, which):
    mean, inverse, gain, shift = norm_rows(table_ref, which)
    mean_grad, mean_cross = back_means(sums, gain, total_ref.shape[0])

    def back(rows):
        normed = (read(rows) - mean) * inverse
        return inverse * (total_ref[rows, :] * gain - mean_grad - normed * mean_cross)

    return back


def turn_kernel(
    grad_ref, mask_ref, weights_ref, middle_ref, table_ref, total_ref, sums_ref, taps_ref, *, cols
):
    sums_ref[0:8, :], sums_ref[8:16, :] = conv_back(
        grad_ref,
        weights_ref.at[1],
        mask_ref,
        taps_ref,
        total_ref,
        lambda rows: middle_ref[rows, :],
        table_ref,
        1,
        cols,
    )


def norm_rows(table_ref, which):
    picks = (2 * which, 2 * which + 1, 6 + which, 9 + which)
    return tuple(table_ref[pick : pick + 1, :] for pick in picks)


def build_masks(ids_ref, mask_ref, lanes_ref, id_rows_ref, id_cols_ref, cols):
    rows = ids_ref.shape[1]
    for row in range(rows):
        here = ids_ref[0, row]
        place = slice(row * cols, (row + 1) * cols)
        id_rows_ref[place, :] = jnp.full((cols, LANES), here, jnp.int32)
        for side, other in ((0, row - 1), (1, row + 1)):
            same = jnp.float32(0.0)
            if 0 <= other < rows:
                same = jnp.where(ids_ref[0, other] == here, 1.0, 0.0).astype(jnp.float32)
            mask_ref[side, place, :] = jnp.full((cols, LANES), same, jnp.float32)
    lane = lax.broadcasted_iota(jnp.int32, (8, LANES), 1)
    each = LANES // cols
    for block in range(rows // each):
        ids = jnp.full((8, LANES), ids_ref[0, block * each], jnp.int32)
        for step in range(1, each):
            ids = jnp.where(lane >= step * cols, ids_ref[0, block * each + step], ids)
        id_cols_ref[:, block * LANES : (block + 1) * LANES] = ids
    ids = id_cols_ref[...].astype(jnp.float32)
    pixels = ids.shape[1]
    pixel = lax.broadcasted_iota(jnp.int32, ids.shape, 1)
    above = jnp.where(pixel < cols, -1.0, pltpu.roll(ids, cols, 1))
    below = jnp.where(pixel >= pixels - cols, -1.0, pltpu.roll(ids, pixels - cols, 1))
    lanes_ref[0:1, :] = jnp.where(above == ids, 1.0, 0.0)[0:1]
    lanes_ref[1:2, :] = jnp.where(below == ids, 1.0, 0.0)[0:1]


def place_pieces(pieces, whole_ref, sems):
    own_pixels = whole_ref.shape[0] // len(pieces)
    height = lax.axis_index("height")
    copies = []
    for place, piece in enumerate(pieces):
        start = pl.multiple_of((height ^ place) * own_pixels, own_pixels)
        rows = pl.ds(start, own_pixels)
        copies.append(pltpu.make_async_copy(piece, whole_ref.at[rows, :], sems.at[place]))
    return copies


def conv_kernel(*refs, cols, count):
    pieces, refs = refs[:count], refs[count:]
    (
        ids_hbm,
        gains_hbm,
        shifts_hbm,
        biases_hbm,
        weights_hbm,
        qkv_hbm,
        proj_hbm,
        features_ref,
        act_one_ref,
        middle_ref,
        act_two_ref,
        residual_ref,
        table_ref,
        mask_ref,
        lanes_ref,
        id_rows_ref,
        id_cols_ref,
        turned_ref,
        qkv_ref,
        proj_ref,
        ids_ref,
        gains_ref,
        shifts_ref,
        biases_ref,
        weights_ref,
        taps_ref,
        own_ref,
        sems,
        piece_sem,
    ) = refs
    pixels, channels = features_ref.shape
    wide = jnp.float32
    turned = [
        (
            weights_hbm.at[which, 2 - row_tap, 2 - col_tap],
            turned_ref.at[which, row_tap, :, col_tap * channels : (col_tap + 1) * channels],
        )
        for which in (1, 0)
        for row_tap in range(3)
        for col_tap in range(3)
    ]
    moves = [
        (ids_hbm, ids_ref),
        (gains_hbm, gains_ref),
        (shifts_hbm, shifts_ref),
        (weights_hbm.at[0], weights_ref.at[0]),
        (biases_hbm, biases_ref),
        (weights_hbm.at[1], weights_ref.at[1]),
        (qkv_hbm, qkv_ref),
        (proj_hbm, proj_ref),
    ] + turned
    copies = [
        pltpu.make_async_copy(source, target, sems.at[index])
        for index, (source, target) in enumerate(moves)
    ]
    own_copy = pltpu.make_async_copy(pieces[0], own_ref, piece_sem)
    for copy in [own_copy] + copies[:6]:
        copy.start()
    clear_edges(taps_ref, cols)

    def read_input(rows):
        return features_ref[rows, :].astype(wide)

    def read_middle(rows):
        return middle_ref[rows, :]

    height = lax.axis_index("height")
    own_pixels = pixels // count
    seen = RunningStats()
    for place in list(range(1, count)) + [0]:
        if place == 0:
            own_copy.wait()
        piece = (pieces[place] if place else own_ref)[...]
        start = pl.multiple_of((height ^ place) * own_pixels, own_pixels)
        features_ref[pl.ds(start, own_pixels), :] = piece
        seen.add(piece.astype(wide))
    table_ref[0:1, :], table_ref[1:2, :] = seen.finish(pixels)
    copies[0].wait()
    build_masks(ids_ref, mask_ref, lanes_ref, id_rows_ref, id_cols_ref, cols)
    copies[1].wait()
    copies[2].wait()
    table_ref[6:9, :] = gains_ref[...]
    table_ref[9:12, :] = shifts_ref[...]
    for copy in copies[6:]:
        copy.start()
    copies[3].wait()
    copies[4].wait()
    seen = RunningStats()

    def keep(rows, value):
        seen.add(value)
        return value

    run_conv(
        taps_ref,
        product_forward(weights_ref.at[0]),
        mask_ref,
        middle_ref,
        activation(read_input, *norm_rows(table_ref, 0), act_one_ref, taps_ref, cols),
        lambda rows, part: part + biases_ref[0:1, :],
        keep,
        cols,
    )
    table_ref[2:3, :], table_ref[3:4, :] = seen.finish(pixels)
    copies[5].wait()
    seen = RunningStats()
    run_conv(
        taps_ref,
        product_forward(weights_ref.at[1]),
        mask_ref,
        residual_ref,
        activation(read_middle, *norm_rows(table_ref, 1), act_two_ref, taps_ref, cols),
        lambda rows, part: part + (read_input(rows) + biases_ref[1:2, :]),
        keep,
        cols,
    )
    table_ref[4:5, :], table_ref[5:6, :] = seen.finish(pixels)
    for copy in copies[6:]:
        copy.wait()


def score_kernel(
    qv_bias_hbm,
    proj_bias_hbm,
    qkv_ref,
    proj_ref,
    residual_ref,
    table_ref,
    id_rows_ref,
    id_cols_ref,
    normed_ref,
    query_ref,
    key_ref,
    value_ref,
    soft_ref,
    out_flip_ref,
    output_ref,
    qv_bias_ref,
    proj_bias_ref,
    value_flip_ref,
    sems,
    *,
    score_scale,
):
    pixels, channels = residual_ref.shape
    own_pixels = output_ref.shape[0]
    wide = jnp.float32
    exponent = score_scale * 1.4426950408889634
    moves = [(qv_bias_hbm, qv_bias_ref), (proj_bias_hbm, proj_bias_ref)]
    copies = [
        pltpu.make_async_copy(source, target, sems.at[index])
        for index, (source, target) in enumerate(moves)
    ]
    for copy in copies:
        copy.start()
    mean, inverse, gain, shift = norm_rows(table_ref, 2)
    scale = inverse * gain
    for copy in copies:
        copy.wait()
    block = min(QUERY_ROWS, pixels)

    def project(index, carry):
        rows = pl.ds(pl.multiple_of(index * block, block), block)
        normed = ((residual_ref[rows, :] - mean) * scale + shift).astype(jnp.bfloat16)
        normed_ref[rows, :] = normed
        query_ref[rows, :] = (
            jnp.dot(normed, qkv_ref[:, 0:channels], preferred_element_type=wide)
            + qv_bias_ref[0:1, :]
        ).astype(jnp.bfloat16)
        key_ref[rows, :] = jnp.dot(
            normed, qkv_ref[:, channels : 2 * channels], preferred_element_type=wide
        ).astype(jnp.bfloat16)
        values = (
            jnp.dot(normed, qkv_ref[:, 2 * channels :], preferred_element_type=wide)
            + qv_bias_ref[1:2, :]
        ).astype(jnp.bfloat16)
        value_ref[rows, :] = values
        value_flip_ref[:, rows] = values.T
        return carry

    lax.fori_loop(0, pixels // block, project, 0)

    def attend(index, carry):
        rows = pl.ds(pl.multiple_of(index * block, block), block)
        scores = lax.dot_general(
            key_ref[...], query_ref[rows, :], (((1,), (1,)), ((), ())), preferred_element_type=wide
        )
        same = widen(id_rows_ref[...], block) == id_cols_ref[0:1, rows]
        scores = jnp.where(same, scores, masked_score)
        scores = jnp.exp2((scores - jnp.max(scores, axis=0, keepdims=True)) * exponent)
        weights = scores * (1.0 / jnp.sum(scores, axis=0, keepdims=True))
        rounded = weights.astype(jnp.bfloat16)
        soft_ref[:, rows] = rounded
        out_flip_ref[:, rows] = jnp.dot(
            value_flip_ref[...], rounded, preferred_element_type=wide
        ).astype(jnp.bfloat16)
        return carry

    lax.fori_loop(0, pixels // block, attend, 0)
    height = lax.axis_index("height")
    own = pl.ds(pl.multiple_of(height * own_pixels, own_pixels), own_pixels)
    output_ref[...] = (
        residual_ref[own, :]
        + lax.dot_general(
            out_flip_ref[:, own],
            proj_ref[...],
            (((0,), (0,)), ((), ())),
            preferred_element_type=wide,
        )
        + proj_bias_ref[...]
    ).astype(jnp.bfloat16)


def own_quarter():
    height = lax.axis_index("height")
    return (height & 1) * 2 + ((height >> 1) & 1)


def send_order(source_ref, targets, axis, share):
    me = lax.axis_index("canvas")
    for step, target in enumerate(targets):
        place = pl.ds(pl.multiple_of((me ^ step) * share, share), share)
        target[...] = source_ref[place, :] if axis == 0 else source_ref[:, place]


def attention_kernel(
    proj_ref,
    normed_ref,
    query_ref,
    key_ref,
    value_ref,
    soft_ref,
    out_flip_ref,
    *refs,
    score_scale,
    count,
):
    pieces, (grad_ref, packed_ref, sums_ref), refs = (
        refs[:count],
        refs[count : count + 3],
        refs[count + 3 :],
    )
    *mixed_refs, mixed_ref, key_flip_ref, back_ref, score_grad_ref, flip_ref, sems = refs
    pixels, channels = normed_ref.shape
    block = min(QUERY_ROWS, pixels)
    wide = jnp.float32
    copies = place_pieces(pieces, grad_ref, sems)
    for copy in copies:
        copy.start()
    quarter = channels // 4
    own = pl.ds(pl.multiple_of(own_quarter() * quarter, quarter), quarter)
    flip_ref[...] = normed_ref[:, own].T
    key_flip_ref[...] = key_ref[...].T
    for copy in copies:
        copy.wait()

    for start in range(0, pixels, block):
        rows = slice(start, start + block)
        back_ref[rows, :] = lax.dot_general(
            grad_ref[rows, :], proj_ref[...], (((1,), (1,)), ((), ())), preferred_element_type=wide
        ).astype(jnp.bfloat16)
    for start in range(0, pixels, block):
        rows = slice(start, start + block)
        weights = soft_ref[:, rows].astype(wide)
        weight_grad = lax.dot_general(
            value_ref[...],
            back_ref[rows, :],
            (((1,), (1,)), ((), ())),
            preferred_element_type=wide,
        )
        dots = jnp.sum(weights * weight_grad, axis=0, keepdims=True)
        score_grad = (weights * (weight_grad - dots)).astype(jnp.bfloat16)
        score_grad_ref[:, rows] = score_grad
        query_grad = jnp.dot(key_flip_ref[...], score_grad, preferred_element_type=wide)
        packed_ref[rows, 0:channels] = (query_grad * score_scale).astype(jnp.bfloat16).T
        packed_ref[rows, 2 * channels :] = jnp.dot(
            soft_ref[rows, :], back_ref[...], preferred_element_type=wide
        ).astype(jnp.bfloat16)
    for start in range(0, pixels, block):
        rows = slice(start, start + block)
        packed_ref[rows, channels : 2 * channels] = (
            jnp.dot(score_grad_ref[rows, :], query_ref[...], preferred_element_type=wide)
            * score_scale
        ).astype(jnp.bfloat16)

    def pack(rows, carry):
        return (
            carry[0] + fold(packed_ref[rows, 0:channels].astype(wide)),
            carry[1] + fold(packed_ref[rows, 2 * channels :].astype(wide)),
            carry[2] + fold(grad_ref[rows, :].astype(wide)),
        )

    zeros = jnp.zeros((8, channels), wide)
    totals = each_chunk(pixels, pack, (zeros, zeros, zeros))
    sums_ref[...] = jnp.zeros(sums_ref.shape, wide)
    for row, total in enumerate(totals):
        sums_ref[8 + row : 9 + row, :] = column_total(total)
    mixed_ref[:, 0 : 3 * channels] = jnp.dot(
        flip_ref[...], packed_ref[...], preferred_element_type=wide
    ).astype(jnp.bfloat16)
    mixed_ref[:, 3 * channels :] = jnp.dot(
        out_flip_ref[own, :], grad_ref[...], preferred_element_type=wide
    ).astype(jnp.bfloat16)
    send_order(mixed_ref, mixed_refs, 0, quarter // len(mixed_refs))


def third_kernel(
    qkv_ref,
    grad_ref,
    packed_ref,
    residual_ref,
    table_ref,
    act_two_ref,
    lanes_ref,
    old_sums_ref,
    residual_grad_ref,
    grad_two_ref,
    sums_ref,
    part_ref,
    total_ref,
    flip_ref,
    columns_ref,
    *,
    cols,
):
    pixels, channels = residual_ref.shape
    block = min(CONV_ROWS, pixels)
    wide = jnp.float32
    mean, inverse, gain, shift = norm_rows(table_ref, 2)
    zeros = jnp.zeros((8, channels), wide)

    sums = (zeros, zeros)
    for start in range(0, pixels, block):
        rows = pl.ds(start, block)
        normed_grad = lax.dot_general(
            packed_ref[rows, :], qkv_ref[...], (((1,), (1,)), ((), ())), preferred_element_type=wide
        )
        total_ref[rows, :] = normed_grad
        normed = (residual_ref[rows, :] - mean) * inverse
        sums = sums[0] + fold(normed_grad), sums[1] + fold(normed_grad * normed)
    sums_ref[...] = old_sums_ref[...]
    sums_ref[5:6, :] = column_total(sums[1])
    sums_ref[6:7, :] = column_total(sums[0])
    mean_grad, mean_cross = back_means(sums, gain, pixels)

    def finish(rows, carry):
        normed = (residual_ref[rows, :] - mean) * inverse
        back = inverse * (total_ref[rows, :] * gain - mean_grad - normed * mean_cross)
        total = grad_ref[rows, :].astype(wide) + back
        residual_grad_ref[rows, :] = total
        low = total.astype(jnp.bfloat16)
        grad_two_ref[rows, :] = low
        return carry + fold(low.astype(wide))

    sums_ref[7:8, :] = column_total(each_chunk(pixels, finish, zeros))
    weight_part(act_two_ref, grad_two_ref, lanes_ref, flip_ref, columns_ref, part_ref, cols)


def second_kernel(
    total_ref,
    partial_ref,
    middle_ref,
    table_ref,
    act_one_ref,
    lanes_ref,
    old_sums_ref,
    part_two_ref,
    grad_one_ref,
    sums_ref,
    keep_one_ref,
    send_one_ref,
    keep_two_ref,
    send_two_ref,
    flip_ref,
    columns_ref,
    part_ref,
    *,
    cols,
):
    pixels, channels = middle_ref.shape
    sums = partial_ref[0:8, :], partial_ref[8:16, :]
    back = norm_back(total_ref, sums, lambda rows: middle_ref[rows, :], table_ref, 1)
    sums_ref[...] = old_sums_ref[...]
    sums_ref[2:3, :] = column_total(sums[1])
    sums_ref[3:4, :] = column_total(sums[0])

    def finish(rows, carry):
        low = back(rows).astype(jnp.bfloat16)
        grad_one_ref[rows, :] = low
        return carry + fold(low.astype(jnp.float32))

    zeros = jnp.zeros((8, channels), jnp.float32)
    sums_ref[4:5, :] = column_total(each_chunk(pixels, finish, zeros))
    weight_part(act_one_ref, grad_one_ref, lanes_ref, flip_ref, columns_ref, part_ref, cols)
    me = lax.axis_index("canvas")
    rows = part_ref.shape[0]
    for source_ref, near, far, keep_ref, send_ref in (
        (part_ref, 1, 2, keep_one_ref, send_one_ref),
        (part_two_ref, 2, 1, keep_two_ref, send_two_ref),
    ):
        width = keep_ref.shape[1]
        for target_ref, flip in ((keep_ref, 0), (send_ref, near)):
            for slot in range(2):
                owner = me ^ flip ^ (slot * far)
                place = pl.ds(pl.multiple_of(owner * width, width), width)
                target_ref[slot * rows : (slot + 1) * rows, :] = source_ref[:, place]


def first_kernel(
    grad_one_ref,
    features_ref,
    residual_grad_ref,
    table_ref,
    mask_ref,
    old_sums_ref,
    weights_ref,
    input_grad_ref,
    sums_ref,
    taps_ref,
    total_ref,
    *,
    cols,
):
    def read(rows):
        return features_ref[rows, :].astype(jnp.float32)

    sums = conv_back(
        grad_one_ref, weights_ref.at[0], mask_ref, taps_ref, total_ref, read, table_ref, 0, cols
    )
    back = norm_back(total_ref, sums, read, table_ref, 0)
    sums_ref[...] = old_sums_ref[...]
    sums_ref[0:1, :] = column_total(sums[1])
    sums_ref[1:2, :] = column_total(sums[0])
    count = input_grad_ref.shape[0]
    own = pl.ds(pl.multiple_of(lax.axis_index("height") * count, count), count)
    input_grad_ref[...] = (residual_grad_ref[own, :] + back(own)).astype(jnp.bfloat16)


def place_kernel(*refs):
    joints, (qkv_hbm, proj_hbm, packed_ref, qkv_ref, proj_ref, sems) = refs[:-6], refs[-6:]
    share = packed_ref.shape[0] // len(joints)
    me = lax.axis_index("canvas")
    for step, joint in enumerate(joints):
        place = pl.ds(pl.multiple_of((me ^ step) * share, share), share)
        packed_ref[place, :] = joint[...]
    spread_quarters([packed_ref], 0, qkv_ref, proj_ref, qkv_hbm, proj_hbm, sems)


def spread_quarters(packed, offset, qkv_ref, proj_ref, qkv_hbm, proj_hbm, sems):
    quarter = packed[0].shape[0]
    inner = qkv_ref.shape[2]
    copies = []
    for index, packed_ref in enumerate(packed):
        owner = own_quarter() ^ (index + offset)
        rows = pl.ds(pl.multiple_of(owner * quarter, quarter), quarter)
        qkv_ref[index] = packed_ref[:, 0:inner].astype(jnp.float32)
        proj_ref[index] = packed_ref[:, inner:].astype(jnp.float32)
        for which, (held, target) in enumerate(((qkv_ref, qkv_hbm), (proj_ref, proj_hbm))):
            copy = pltpu.make_async_copy(held.at[index], target.at[rows, :], sems.at[index, which])
            copy.start()
            copies.append(copy)
    for copy in copies:
        copy.wait()


def join_kernel(*refs):
    ins, (qkv_hbm, proj_hbm, qkv_ref, proj_ref, sems) = refs[:-5], refs[-5:]
    packed = ins[2:]
    spread_quarters(packed, 1, qkv_ref, proj_ref, qkv_hbm, proj_hbm, sems)


def halve_kernel(
    keep_one_ref,
    got_one_ref,
    keep_two_ref,
    got_two_ref,
    hold_one_ref,
    send_one_ref,
    hold_two_ref,
    send_two_ref,
):
    for keep_ref, got_ref, hold_ref, send_ref in (
        (keep_one_ref, got_one_ref, hold_one_ref, send_one_ref),
        (keep_two_ref, got_two_ref, hold_two_ref, send_two_ref),
    ):
        total = keep_ref[...].astype(jnp.float32) + got_ref[...].astype(jnp.float32)
        rows = hold_ref.shape[0]
        hold_ref[...] = total[0:rows]
        send_ref[...] = total[rows:].astype(jnp.bfloat16)


def sums_kernel(
    sums_ref,
    got_sums_ref,
    hold_one_ref,
    got_one_ref,
    hold_two_ref,
    got_two_ref,
    share_ref,
    gains_ref,
    shifts_ref,
    conv_ref,
    qv_ref,
    proj_ref,
):
    for which, (hold_ref, got_ref) in enumerate(
        ((hold_one_ref, got_one_ref), (hold_two_ref, got_two_ref))
    ):
        total = hold_ref[...] + got_ref[...].astype(jnp.float32)
        share_ref[which] = total.reshape(share_ref.shape[1:])
    total = sums_ref[...] + got_sums_ref[...]
    for row, start in enumerate((0, 2, 5)):
        gains_ref[row : row + 1, :] = total[start : start + 1]
        shifts_ref[row : row + 1, :] = total[start + 1 : start + 2]
    conv_ref[0:1, :] = total[4:5]
    conv_ref[1:2, :] = total[7:8]
    qv_ref[...] = total[8:10]
    proj_ref[...] = total[10:11]


def call_kernel(kernel, outputs, scratch, operands, places, flops, limit, out_places=None, aliases={}):
    out_places = out_places or "v" * len(outputs)
    spaces = {
        "v": pl.BlockSpec(memory_space=pltpu.VMEM),
        "s": pl.BlockSpec(memory_space=pltpu.SMEM),
        "h": pl.BlockSpec(memory_space=pl.ANY),
        "o": pl.BlockSpec(memory_space=pltpu.VMEM),
        "a": pl.BlockSpec(memory_space=pl.ANY),
    }
    moved = 8 * flops // LANES
    held = {"v": pltpu.VMEM, "h": pltpu.HBM, "o": jax.ShapeDtypeStruct}
    operands = [
        pltpu.with_memory_space_constraint(array, pltpu.HBM) if place == "h" else array
        for array, place in zip(operands, places)
    ]
    return pl.pallas_call(
        kernel,
        out_shape=[held[place](*output) for output, place in zip(outputs, out_places)],
        in_specs=[spaces[place] for place in places],
        out_specs=[spaces[place] for place in out_places],
        scratch_shapes=scratch,
        input_output_aliases=aliases,
        compiler_params=pltpu.CompilerParams(vmem_limit_bytes=limit * 2**20),
        cost_estimate=pl.CostEstimate(flops=flops, bytes_accessed=moved, transcendentals=0),
    )(*operands)


def send_height(block, step):
    size = lax.axis_size("height")
    return lax.ppermute(block, "height", [(i, i ^ step) for i in range(size)])


def with_cores(blocks):
    return [piece for block in blocks for piece in (block, send_height(block, 1))]


def send_canvas(block, step):
    size = lax.axis_size("canvas")
    return lax.ppermute(block, "canvas", [(i, i ^ step) for i in range(size)])


def trade_canvas(pieces):
    return [pieces[0]] + [send_canvas(piece, step) for step, piece in enumerate(pieces) if step]


def whole_canvas(
    features,
    tile_ids,
    norm_gains,
    norm_shifts,
    conv_weights,
    conv_biases,
    qkv_weight,
    qv_bias,
    proj_weight,
    proj_bias,
    cotangent,
):
    height_size = lax.axis_size("height")
    canvas_size = lax.axis_size("canvas")
    local_rows, cols, channels = features.shape[1:]
    all_rows = tile_ids.shape[1]
    pixels = all_rows * cols
    own_pixels = local_rows * cols
    out_share = channels // height_size
    ci_share = channels // canvas_size
    quarter = channels // 4
    row_share = quarter // canvas_size
    low, wide = jnp.bfloat16, jnp.float32

    own_features = features.reshape(own_pixels, channels)
    own_grad = cotangent.reshape(own_pixels, channels)
    steps = range(2, height_size, 2)
    held_features = [own_features] + [send_height(own_features, step) for step in steps]
    pieces = with_cores(held_features)
    near_grad, pieces[2] = lax.optimization_barrier((own_grad, held_features[1]))
    far_grad, *pieces[4::2] = lax.optimization_barrier((own_grad, *held_features[2:]))
    held_grads = [own_grad, send_height(near_grad, 2)]
    held_grads += [send_height(far_grad, step) for step in steps[1:]]

    plane = ((pixels, channels), low)
    plane_wide = ((pixels, channels), wide)
    sums_shape = ((16, channels), wide)
    mixed_shapes = [((row_share, 4 * channels), low)] * canvas_size
    taps = pltpu.VMEM((pixels + 2 * cols, 3 * channels), low)
    held_wide = pltpu.VMEM((pixels, channels), wide)
    flipped = pltpu.VMEM((channels, pixels), low)
    narrow = pltpu.VMEM((NARROW, pixels), low)
    columns = pltpu.VMEM((9 * out_share, pixels), low)
    part_held = pltpu.VMEM((9 * out_share, channels), low)
    sem = pltpu.SemaphoreType.DMA
    conv_flops = 2 * 9 * pixels * channels * channels
    dot_flops = 2 * pixels * channels * channels
    score_flops = 2 * pixels * pixels * channels
    scale = channels ** (-0.5)

    (
        all_features,
        act_one,
        middle,
        act_two,
        residual,
        table,
        mask,
        lane_mask,
        id_rows,
        id_cols,
        turned,
        held_qkv,
        held_proj,
    ) = call_kernel(
        functools.partial(conv_kernel, cols=cols, count=height_size),
        [
            plane,
            plane,
            plane_wide,
            plane,
            plane_wide,
            ((16, channels), wide),
            ((2, pixels, LANES), wide),
            ((8, pixels), wide),
            ((pixels, LANES), jnp.int32),
            ((8, pixels), jnp.int32),
            ((2, 3, channels, 3 * channels), low),
            (qkv_weight.shape, low),
            (proj_weight.shape, low),
        ],
        [
            pltpu.SMEM(tile_ids.shape, jnp.int32),
            pltpu.VMEM(norm_gains.shape, wide),
            pltpu.VMEM(norm_shifts.shape, wide),
            pltpu.VMEM(conv_biases.shape, wide),
            pltpu.VMEM(conv_weights.shape, low),
            taps,
            pltpu.VMEM((own_pixels, channels), low),
            sem((26,)),
            sem,
        ],
        [
            *pieces,
            tile_ids,
            norm_gains,
            norm_shifts,
            conv_biases,
            conv_weights,
            qkv_weight,
            proj_weight,
        ],
        "h" + "v" * (height_size - 1) + "h" * 7,
        2 * conv_flops,
        24,
    )
    residual, *held_grads = lax.optimization_barrier((residual, *held_grads))
    grad_pieces = with_cores(held_grads)
    normed, query, key, value, soft, out_flip, output = call_kernel(
        functools.partial(score_kernel, score_scale=scale),
        [
            plane,
            plane,
            plane,
            plane,
            ((pixels, pixels), low),
            ((channels, pixels), low),
            ((own_pixels, channels), low),
        ],
        [
            pltpu.VMEM(qv_bias.shape, wide),
            pltpu.VMEM((1, channels), wide),
            flipped,
            sem((2,)),
        ],
        [
            qv_bias,
            proj_bias.reshape(1, channels),
            held_qkv,
            held_proj,
            residual,
            table,
            id_rows,
            id_cols,
        ],
        "hhvvvvvv",
        3 * dot_flops + 2 * score_flops,
        16,
        "v" * 6 + "o",
    )
    normed, *grad_pieces = lax.optimization_barrier((normed, *grad_pieces))
    all_grad, packed, sums, *mixed = call_kernel(
        functools.partial(attention_kernel, score_scale=scale, count=height_size),
        [plane, ((pixels, 3 * channels), low), sums_shape, *mixed_shapes],
        [
            pltpu.VMEM((quarter, 4 * channels), low),
            flipped,
            pltpu.VMEM((pixels, channels), low),
            pltpu.VMEM((pixels, pixels), low),
            pltpu.VMEM((quarter, pixels), low),
            sem((height_size,)),
        ],
        [held_proj, normed, query, key, value, soft, out_flip, *grad_pieces],
        "vvvvvvvh" + "a" * (height_size - 1),
        3 * dot_flops + 4 * score_flops,
        20,
    )
    mixed = trade_canvas(mixed)
    residual_grad, grad_two, sums, part_two = call_kernel(
        functools.partial(third_kernel, cols=cols),
        [plane_wide, plane, sums_shape, ((9 * out_share, channels), low)],
        [held_wide, narrow, columns],
        [held_qkv, all_grad, packed, residual, table, act_two, lane_mask, sums],
        "vvvvvvvv",
        3 * dot_flops + conv_flops // height_size,
        16,
    )
    grad_two, *mixed = lax.optimization_barrier((grad_two, *mixed))
    mixed_sum = mixed[0].astype(wide)
    for piece in mixed[1:]:
        mixed_sum = mixed_sum + piece.astype(wide)
    joints = trade_canvas([mixed_sum.astype(low)] * canvas_size)
    act_two_grad, partial_sums = call_kernel(
        functools.partial(turn_kernel, cols=cols),
        [plane_wide, sums_shape],
        [taps],
        [grad_two, mask, turned, middle, table],
        "vvvvv",
        conv_flops,
        16,
    )
    act_two_grad, *joints = lax.optimization_barrier((act_two_grad, *joints))
    qkv_grad, proj_grad, own_mixed = call_kernel(
        place_kernel,
        [(qkv_weight.shape, wide), (proj_weight.shape, wide), ((quarter, 4 * channels), low)],
        [
            pltpu.VMEM((1, quarter, 3 * channels), wide),
            pltpu.VMEM((1, quarter, channels), wide),
            sem((1, 2)),
        ],
        joints,
        "v" * canvas_size,
        0,
        12,
        "hhv",
    )
    chip_mixed = send_height(own_mixed, 2)
    core_mixed = send_height(own_mixed, 1)
    grad_one, sums, keep_one, send_one, keep_two, send_two = call_kernel(
        functools.partial(second_kernel, cols=cols),
        [plane, sums_shape] + [((18 * out_share, ci_share), low)] * 4,
        [narrow, columns, part_held],
        [act_two_grad, partial_sums, middle, table, act_one, lane_mask, sums, part_two],
        "vvvvvvvv",
        conv_flops // height_size,
        16,
    )
    got_one, got_two = send_canvas(send_one, 1), send_canvas(send_two, 2)
    input_grad, sums = call_kernel(
        functools.partial(first_kernel, cols=cols),
        [((own_pixels, channels), low), sums_shape],
        [taps, held_wide],
        [grad_one, all_features, residual_grad, table, mask, sums, turned],
        "vvvvvvv",
        0,
        16,
        "ov",
    )
    sums, chip_mixed, core_mixed, got_one, got_two = lax.optimization_barrier(
        (sums, chip_mixed, core_mixed, got_one, got_two)
    )
    got_sums = send_canvas(sums, 1)
    hold_one, send_one, hold_two, send_two = call_kernel(
        halve_kernel,
        [((9 * out_share, ci_share), kind) for kind in (wide, low, wide, low)],
        [],
        [keep_one, got_one, keep_two, got_two],
        "vvvv",
        0,
        12,
    )
    got_one, got_two = send_canvas(send_one, 2), send_canvas(send_two, 1)
    both_mixed = send_height(chip_mixed, 1)
    sums = sums + got_sums
    got_sums = send_canvas(sums, 2)
    qkv_grad, proj_grad = call_kernel(
        join_kernel,
        [(qkv_weight.shape, wide), (proj_weight.shape, wide)],
        [
            pltpu.VMEM((3, quarter, 3 * channels), wide),
            pltpu.VMEM((3, quarter, channels), wide),
            sem((3, 2)),
        ],
        [qkv_grad, proj_grad, chip_mixed, core_mixed, both_mixed],
        "hhvvv",
        0,
        12,
        "hh",
        {0: 0, 1: 1},
    )
    qkv_grad, got_sums, got_one, got_two = lax.optimization_barrier(
        (qkv_grad, got_sums, got_one, got_two)
    )
    vector_shapes = [norm_gains.shape, norm_shifts.shape, conv_biases.shape, qv_bias.shape]
    conv_grad, gains_grad, shifts_grad, biases_grad, qv_grad, proj_bias_grad = call_kernel(
        sums_kernel,
        [((2, 3, 3, out_share, ci_share), wide)]
        + [(shape, wide) for shape in vector_shapes + [(1, channels)]],
        [],
        [sums, got_sums, hold_one, got_one, hold_two, got_two],
        "vvvvvv",
        0,
        12,
        "o" * 6,
    )
    own_shape = (1, local_rows, cols, channels)
    return (
        output.reshape(own_shape),
        input_grad.reshape(own_shape),
        gains_grad,
        shifts_grad,
        jnp.swapaxes(conv_grad, 3, 4),
        biases_grad,
        qkv_grad,
        qv_grad,
        proj_grad,
        proj_bias_grad.reshape(channels),
    )


def on_device(*arrays):
    features, tile_ids = arrays[0], arrays[1]
    local_rows, cols, channels = features.shape[1:]
    pixels = tile_ids.shape[1] * cols
    height_size, canvas_size = lax.axis_size("height"), lax.axis_size("canvas")
    powers = all(size & (size - 1) == 0 for size in (height_size, canvas_size, cols))
    fits = (
        powers
        and height_size > 2
        and canvas_size == 4
        and channels == LANES * canvas_size
        and pixels <= MOST_PIXELS
        and pixels % min(CONV_ROWS, pixels) == 0
        and pixels % FILL_ROWS == 0
        and FILL_ROWS % CHUNK == 0
        and (local_rows * cols) % LANES == 0
        and CHUNK % cols == 0
        and cols % 16 == 0
        and channels % (LANES * canvas_size) == 0
        and 2 * channels == NARROW * height_size
    )
    return whole_canvas(*arrays) if fits else split_canvas(*arrays)


def solution(mesh):
    in_specs = (
        P("canvas", "height", None, None),
        P("canvas", None),
        P(),
        P(),
        P(),
        P(),
        P(),
        P(),
        P(),
        P(),
        P("canvas", "height", None, None),
    )
    out_specs = (
        P("canvas", "height", None, None),
        P("canvas", "height", None, None),
        P(),
        P(),
        P(None, None, None, "canvas", "height"),
        P(),
        P(),
        P(),
        P(),
        P(),
    )
    return jax.shard_map(
        on_device, mesh=mesh, in_specs=in_specs, out_specs=out_specs, check_vma=False
    )
```

```python
import functools

import jax
import jax.numpy as jnp
from jax import lax
from jax.experimental import pallas as pl
from jax.experimental.pallas import tpu as pltpu
from jax.sharding import PartitionSpec as P

GROUPS = 32


epsilon = 1e-06
masked_score = -1e30
MOST_PIXELS = 1024
LANES = 128
NARROW = 128
CHUNK = 128
CONV_ROWS = 256
QUERY_ROWS = 512


def extended(block, sides, width):
    for axis, dim in sides:
        count = lax.axis_size(axis)
        forward = [(i, i + 1) for i in range(count - 1)]
        backward = [(target, source) for source, target in forward]
        low = lax.ppermute(
            lax.slice_in_dim(block, block.shape[dim] - width, None, axis=dim), axis, forward
        )
        high = lax.ppermute(lax.slice_in_dim(block, 0, width, axis=dim), axis, backward)
        block = jnp.concatenate([low, block, high], axis=dim)
    return block


def group_total(vector):
    return vector.reshape(GROUPS, -1).sum(axis=1)


def spread_groups(vector, channels):
    return jnp.repeat(vector, channels // GROUPS)


def norm_forward(values, gain, shift, members):
    channels = values.shape[1]
    totals = lax.psum(group_total(jnp.sum(values, axis=0)), "height")
    centered = values - spread_groups(totals / members, channels)
    squares = lax.psum(group_total(jnp.sum(centered * centered, axis=0)), "height")
    inverse = spread_groups(lax.rsqrt(squares / members + epsilon), channels)
    normed = centered * inverse
    return (normed, inverse, normed * gain + shift)


def norm_backward(grad_in, normed, inverse, gain, members):
    channels = grad_in.shape[1]
    scaled = grad_in * gain
    both_sums = lax.psum(
        (group_total(jnp.sum(scaled, axis=0)), group_total(jnp.sum(scaled * normed, axis=0))),
        "height",
    )
    mean_grad = spread_groups(both_sums[0] / members, channels)
    mean_cross = spread_groups(both_sums[1] / members, channels)
    result = inverse * (scaled - mean_grad - normed * mean_cross)
    return (result, jnp.sum(grad_in * normed, axis=0), jnp.sum(grad_in, axis=0))


def swish(values):
    return values * jax.nn.sigmoid(values)


def swish_slope(values):
    sigmoid_part = jax.nn.sigmoid(values)
    return sigmoid_part * (1.0 + values * (1.0 - sigmoid_part))


def tap_columns(padded, row_mask, local_rows, canvas_cols):
    pieces = []
    for row_tap in range(3):
        rows_taken = padded[row_tap : row_tap + local_rows] * row_mask[:, row_tap, None, None]
        for col_tap in range(3):
            pieces.append(rows_taken[:, col_tap : col_tap + canvas_cols])
    stacked = jnp.concatenate(pieces, axis=2)
    return stacked.reshape(local_rows * canvas_cols, stacked.shape[2])


def conv_forward(acts, row_mask, weight, bias):
    local_rows, canvas_cols, channels = acts.shape
    rimmed = extended(acts, (("height", 0),), 1)
    padded = jnp.pad(rimmed, ((0, 0), (1, 1), (0, 0)))
    gathered = tap_columns(padded, row_mask, local_rows, canvas_cols)
    result = (
        jnp.dot(
            gathered, weight.reshape(9 * channels, channels), preferred_element_type=jnp.float32
        )
        + bias
    )
    return (result, gathered)


def conv_backward(grad_low, row_mask, weight, gathered):
    local_rows, canvas_cols, channels = grad_low.shape
    flat_grad = grad_low.reshape(local_rows * canvas_cols, channels)
    weight_grad = lax.dot_general(
        gathered, flat_grad, (((0,), (0,)), ((), ())), preferred_element_type=jnp.float32
    )
    rimmed = extended(grad_low, (("height", 0),), 1)
    padded = jnp.pad(rimmed, ((0, 0), (1, 1), (0, 0)))
    grad_taps = tap_columns(padded, row_mask, local_rows, canvas_cols)
    flipped = jnp.transpose(weight[::-1, ::-1], (0, 1, 3, 2)).reshape(9 * channels, channels)
    input_part = jnp.dot(grad_taps, flipped, preferred_element_type=jnp.float32)
    return (
        input_part,
        weight_grad.reshape(3, 3, channels, channels),
        jnp.sum(flat_grad.astype(jnp.float32), axis=0),
    )


def take_rows(array, offset, count):
    return lax.dynamic_slice_in_dim(array, offset, count)


def score_grads(
    queries, out_grad, log_total, row_dots, query_ids, key_rows, value_rows, key_ids, score_scale
):
    scores = (
        lax.dot_general(
            queries, key_rows, (((1,), (1,)), ((), ())), preferred_element_type=jnp.float32
        )
        * score_scale
    )
    same_tile = query_ids[:, None] == key_ids[None, :]
    softmax_block = jnp.exp(jnp.where(same_tile, scores - log_total[:, None], masked_score))
    weight_grad = lax.dot_general(
        out_grad, value_rows, (((1,), (1,)), ((), ())), preferred_element_type=jnp.float32
    )
    score_grad = (softmax_block * (weight_grad - row_dots[:, None])).astype(jnp.bfloat16)
    return (softmax_block.astype(jnp.bfloat16), score_grad)


def split_canvas(
    features,
    tile_ids,
    norm_gains,
    norm_shifts,
    conv_weights,
    conv_biases,
    qkv_weight,
    qv_bias,
    proj_weight,
    proj_bias,
    cotangent,
):
    height_size = lax.axis_size("height")
    local_rows = features.shape[1]
    canvas_cols = features.shape[2]
    channels = features.shape[3]
    pixels = local_rows * canvas_cols
    row_ids = tile_ids[0]
    all_rows = row_ids.shape[0]
    members = float(all_rows * canvas_cols * (channels // GROUPS))
    score_scale = channels ** (-0.5)
    first_row = lax.axis_index("height") * local_rows
    edge_ids = jnp.full((1,), -1, jnp.int32)
    padded_ids = jnp.concatenate([edge_ids, row_ids, edge_ids])
    near_ids = lax.dynamic_slice_in_dim(padded_ids, first_row, local_rows + 2)
    own_rows = near_ids[1 : local_rows + 1]
    row_mask = jnp.stack(
        [near_ids[row_tap : row_tap + local_rows] == own_rows for row_tap in range(3)], axis=1
    ).astype(jnp.bfloat16)
    key_ids = jnp.repeat(row_ids, canvas_cols)
    query_ids = jnp.repeat(own_rows, canvas_cols)
    grid_shape = (local_rows, canvas_cols, channels)
    inputs = features[0].reshape(pixels, channels).astype(jnp.float32)
    normed_one, inverse_one, pre_one = norm_forward(inputs, norm_gains[0], norm_shifts[0], members)
    act_one = swish(pre_one).astype(jnp.bfloat16).reshape(grid_shape)
    middle, taps_one = conv_forward(act_one, row_mask, conv_weights[0], conv_biases[0])
    normed_two, inverse_two, pre_two = norm_forward(middle, norm_gains[1], norm_shifts[1], members)
    act_two = swish(pre_two).astype(jnp.bfloat16).reshape(grid_shape)
    branch, taps_two = conv_forward(act_two, row_mask, conv_weights[1], conv_biases[1])
    residual = inputs + branch
    normed_three, inverse_three, pre_three = norm_forward(
        residual, norm_gains[2], norm_shifts[2], members
    )
    attn_input = pre_three.astype(jnp.bfloat16)
    mixed = jnp.dot(attn_input, qkv_weight, preferred_element_type=jnp.float32)
    queries = (mixed[:, :channels] + qv_bias[0]).astype(jnp.bfloat16)
    key_rows = mixed[:, channels : 2 * channels].astype(jnp.bfloat16)
    value_rows = (mixed[:, 2 * channels :] + qv_bias[1]).astype(jnp.bfloat16)
    running_max = jnp.full((pixels,), masked_score, jnp.float32)
    key_piece = lax.all_gather(key_rows, "height", axis=0, tiled=True)
    value_piece = lax.all_gather(value_rows, "height", axis=0, tiled=True)
    scores = (
        lax.dot_general(
            queries, key_piece, (((1,), (1,)), ((), ())), preferred_element_type=jnp.float32
        )
        * score_scale
    )
    same_tile = query_ids[:, None] == key_ids[None, :]
    scores = jnp.where(same_tile, scores, masked_score)
    new_max = jnp.maximum(running_max, jnp.max(scores, axis=1))
    weights = jnp.where(same_tile, jnp.exp(scores - new_max[:, None]), 0.0)
    summed_out = jnp.dot(
        weights.astype(jnp.bfloat16), value_piece, preferred_element_type=jnp.float32
    )
    total_weight = jnp.sum(weights, axis=1)
    log_total = new_max + jnp.log(total_weight)
    attended = summed_out / total_weight[:, None]
    attended_low = attended.astype(jnp.bfloat16)
    output = (
        residual
        + jnp.dot(attended_low, proj_weight, preferred_element_type=jnp.float32)
        + proj_bias
    )
    out_grad = cotangent[0].reshape(pixels, channels)
    out_grad_full = out_grad.astype(jnp.float32)
    proj_grad = lax.dot_general(
        attended_low, out_grad, (((0,), (0,)), ((), ())), preferred_element_type=jnp.float32
    )
    proj_bias_grad = jnp.sum(out_grad_full, axis=0)
    attended_grad = lax.dot_general(
        out_grad, proj_weight, (((1,), (1,)), ((), ())), preferred_element_type=jnp.float32
    ).astype(jnp.bfloat16)
    row_dots = jnp.sum(attended_grad.astype(jnp.float32) * attended, axis=1)
    block_rows = pixels * min(height_size, 8)
    zero_block = jnp.zeros((pixels, channels), jnp.float32)
    key_all, value_all = (
        lax.all_gather(key_rows, "height", axis=0, tiled=True),
        lax.all_gather(value_rows, "height", axis=0, tiled=True),
    )
    query_all, grad_all = (
        lax.all_gather(queries, "height", axis=0, tiled=True),
        lax.all_gather(attended_grad, "height", axis=0, tiled=True),
    )
    total_all, dots_all = (
        lax.all_gather(log_total, "height", axis=0, tiled=True),
        lax.all_gather(row_dots, "height", axis=0, tiled=True),
    )

    def own_query_step(running, block_index):
        offset = block_index * block_rows
        key_part = take_rows(key_all, offset, block_rows)
        rounded, score_grad = score_grads(
            queries,
            attended_grad,
            log_total,
            row_dots,
            query_ids,
            key_part,
            take_rows(value_all, offset, block_rows),
            take_rows(key_ids, offset, block_rows),
            score_scale,
        )
        return (
            running
            + jnp.dot(score_grad, key_part, preferred_element_type=jnp.float32) * score_scale,
            None,
        )

    def own_key_step(running, block_index):
        offset = block_index * block_rows
        query_part = take_rows(query_all, offset, block_rows)
        grad_part = take_rows(grad_all, offset, block_rows)
        rounded, score_grad = score_grads(
            query_part,
            grad_part,
            take_rows(total_all, offset, block_rows),
            take_rows(dots_all, offset, block_rows),
            take_rows(key_ids, offset, block_rows),
            key_rows,
            value_rows,
            query_ids,
            score_scale,
        )
        key_part = (
            lax.dot_general(
                score_grad, query_part, (((0,), (0,)), ((), ())), preferred_element_type=jnp.float32
            )
            * score_scale
        )
        value_part = lax.dot_general(
            rounded, grad_part, (((0,), (0,)), ((), ())), preferred_element_type=jnp.float32
        )
        return ((running[0] + key_part, running[1] + value_part), None)

    block_count = key_all.shape[0] // block_rows
    query_grad, unused_one = lax.scan(own_query_step, zero_block, jnp.arange(block_count))
    (key_grad, value_grad), unused_two = lax.scan(
        own_key_step, (zero_block, zero_block), jnp.arange(block_count)
    )
    query_low = query_grad.astype(jnp.bfloat16)
    key_low = key_grad.astype(jnp.bfloat16)
    value_low = value_grad.astype(jnp.bfloat16)
    stacked_grad = jnp.concatenate([query_low, key_low, value_low], axis=1)
    qkv_grad = lax.dot_general(
        attn_input, stacked_grad, (((0,), (0,)), ((), ())), preferred_element_type=jnp.float32
    )
    qv_grad = jnp.stack(
        [
            jnp.sum(query_low.astype(jnp.float32), axis=0),
            jnp.sum(value_low.astype(jnp.float32), axis=0),
        ]
    )
    normed_grad = lax.dot_general(
        stacked_grad, qkv_weight, (((1,), (1,)), ((), ())), preferred_element_type=jnp.float32
    )
    back_three, gain_three, shift_three = norm_backward(
        normed_grad, normed_three, inverse_three, norm_gains[2], members
    )
    residual_grad = out_grad_full + back_three
    grad_two = residual_grad.astype(jnp.bfloat16).reshape(grid_shape)
    act_two_grad, weight_two_grad, bias_two_grad = conv_backward(
        grad_two, row_mask, conv_weights[1], taps_two
    )
    middle_grad, gain_two, shift_two = norm_backward(
        act_two_grad * swish_slope(pre_two), normed_two, inverse_two, norm_gains[1], members
    )
    grad_one = middle_grad.astype(jnp.bfloat16).reshape(grid_shape)
    act_one_grad, weight_one_grad, bias_one_grad = conv_backward(
        grad_one, row_mask, conv_weights[0], taps_one
    )
    input_back, gain_one, shift_one = norm_backward(
        act_one_grad * swish_slope(pre_one), normed_one, inverse_one, norm_gains[0], members
    )
    input_grad = residual_grad + input_back
    conv_grad = jnp.stack([weight_one_grad, weight_two_grad])
    conv_part = lax.psum_scatter(conv_grad, "height", scatter_dimension=4, tiled=True)
    conv_part = lax.psum_scatter(
        conv_part.astype(jnp.bfloat16), "canvas", scatter_dimension=3, tiled=True
    ).astype(jnp.float32)
    summed = lax.psum(
        (
            jnp.stack([gain_one, gain_two, gain_three]),
            jnp.stack([shift_one, shift_two, shift_three]),
            jnp.stack([bias_one_grad, bias_two_grad]),
            qkv_grad,
            qv_grad,
            proj_grad,
            proj_bias_grad,
        ),
        ("canvas", "height"),
    )
    return (
        output.astype(jnp.bfloat16).reshape((1,) + grid_shape),
        input_grad.astype(jnp.bfloat16).reshape((1,) + grid_shape),
        summed[0],
        summed[1],
        conv_part,
        summed[2],
        summed[3],
        summed[4],
        summed[5],
        summed[6],
    )


def fold(block):
    rows, width = block.shape
    return jnp.sum(block.reshape(rows // 8, 8, width), axis=0)


def group_lanes(block, group):
    lane = lax.broadcasted_iota(jnp.int32, block.shape, 1)
    width = block.shape[1]
    step = 1
    while step < group:
        above = pltpu.roll(block, step, 1)
        below = pltpu.roll(block, width - step, 1)
        block = block + jnp.where((lane & step) != 0, above, below)
        step *= 2
    return block


def group_mean(partial, members):
    spread = group_lanes(partial, partial.shape[1] // GROUPS)
    return jnp.sum(spread, axis=0, keepdims=True) * (1.0 / members)


def widen(block, width):
    return jnp.concatenate([block] * (width // block.shape[1]), axis=1)


def each_block(pixels, block, body, carry=0):
    def step(index, carry):
        return body(pl.ds(pl.multiple_of(index * block, block), block), carry)

    return lax.fori_loop(0, pixels // block, step, carry)


def each_chunk(pixels, body, carry):
    return each_block(pixels, CHUNK, body, carry)


def aligned(start, step):
    return start if isinstance(start, int) else pl.multiple_of(start, step)


def fold_about(block, center):
    rows, width = block.shape
    offset = block.reshape(rows // 8, 8, width) - center[None]
    return jnp.sum(offset, axis=0), jnp.sum(offset * offset, axis=0)


def finish_stats(center, sums, squares, pixels):
    width = center.shape[1] // GROUPS
    share = pixels / 8.0
    means = center + sums * (1.0 / share)
    spread = squares - sums * sums * (1.0 / share)
    mean = group_mean(means, 8.0 * width)
    offset = means - mean
    variance = group_mean(spread + share * offset * offset, float(pixels * width))
    return mean, lax.rsqrt(variance + epsilon)


class RunningStats:
    def __init__(self):
        self.center = None

    def add(self, block):
        if self.center is None:
            self.center = block[0:8]
            self.sums, self.squares = fold_about(block, self.center)
        else:
            sums, squares = fold_about(block, self.center)
            self.sums, self.squares = self.sums + sums, self.squares + squares

    def finish(self, pixels):
        return finish_stats(self.center, self.sums, self.squares, pixels)


def put_taps(taps_refs, block, rows, cols):
    count, channels = block.shape
    place = lax.broadcasted_iota(jnp.int32, block.shape, 0) & (cols - 1)
    left = jnp.where(place == 0, 0.0, pltpu.roll(block, 1, 0))
    right = jnp.where(place == cols - 1, 0.0, pltpu.roll(block, count - 1, 0))
    taps_ref = taps_refs[rows.start // CONV_ROWS]
    start = rows.start % CONV_ROWS + cols
    inner = slice(start, start + count)
    taps_ref[inner, 0:channels] = left.astype(jnp.bfloat16)
    taps_ref[inner, channels : 2 * channels] = block.astype(jnp.bfloat16)
    taps_ref[inner, 2 * channels :] = right.astype(jnp.bfloat16)


def clear_edges(taps_refs, cols):
    for taps_ref in taps_refs:
        taps_ref[0:cols, :] = jnp.zeros((cols, taps_ref.shape[1]), taps_ref.dtype)


def row_slabs(taps_refs, ids_ref, first, count, shift, cols):
    total = ids_ref.shape[1]
    each = CONV_ROWS // cols
    slabs = []
    for row in range(first, first + count):
        other = row + shift
        if 0 <= other < total:
            place = (other % each + 1) * cols
            if shift:
                place = jnp.where(ids_ref[0, other] == ids_ref[0, row], place, 0)
                place = pl.multiple_of(place, cols)
            slabs.append(taps_refs[other // each][pl.ds(place, cols), :])
        else:
            slabs.append(taps_refs[0][0:cols, :])
    return jnp.concatenate(slabs, axis=0)


def run_conv(taps_refs, ids_ref, product, total_ref, fill, last, cols):
    blocks = len(taps_refs)

    def fill_block(index):
        if index < blocks:
            for start in range(index * CONV_ROWS, (index + 1) * CONV_ROWS, CHUNK):
                fill(pl.ds(start, CHUNK))

    fill_block(0)
    fill_block(1)
    each = CONV_ROWS // cols
    for index in range(blocks):
        fill_block(index + 2)
        near = [row_slabs(taps_refs, ids_ref, index * each, each, shift, cols) for shift in (-1, 0, 1)]
        rows = pl.ds(index * CONV_ROWS, CONV_ROWS)
        total_ref[rows, :] = last(rows, product(jnp.concatenate(near, axis=1)))


def product_forward(weight_ref):
    channels = weight_ref.shape[-1]

    def product(near):
        weights = weight_ref[...].reshape(9 * channels, channels)
        return jnp.dot(near, weights, preferred_element_type=jnp.float32)

    return product


def product_backward(weight_ref):
    def product(near):
        return lax.dot_general(
            near, weight_ref[...], (((1,), (1,)), ((), ())), preferred_element_type=jnp.float32
        )

    return product


def smooth(values):
    part = 0.5 * jnp.tanh(0.5 * values) + 0.5
    return values * part, part


def activation(read, mean, inverse, gain, shift, act_ref, taps_refs, cols):
    scale = inverse * gain

    def fill(rows):
        act = smooth((read(rows) - mean) * scale + shift)[0]
        act_ref[rows, :] = act.astype(jnp.bfloat16)
        put_taps(taps_refs, act, rows, cols)

    return fill


def back_means(sums, gain, pixels):
    channels = gain.shape[1]
    members = float(pixels * (channels // GROUPS))
    return group_mean(sums[0] * gain, members), group_mean(sums[1] * gain, members)


def column_total(partial):
    return jnp.sum(partial, axis=0, keepdims=True)


def weight_part(act_ref, grad_ref, lanes_ref, flip_ref, columns_ref, part_ref, cols):
    pixels, channels = act_ref.shape
    height = lax.axis_index("height")
    share = NARROW // 2
    block = pl.ds(pl.multiple_of((height // 2) * NARROW, NARROW), NARROW)
    flip_ref[...] = grad_ref[:, block].T
    own = pl.ds(pl.multiple_of((height % 2) * share, share), share)
    grad = flip_ref[own, :].astype(jnp.float32)
    place = lax.broadcasted_iota(jnp.int32, grad.shape, 1) & (cols - 1)
    for col_tap in range(3):
        shifted = grad
        if col_tap == 0:
            shifted = jnp.where(place == cols - 1, 0.0, pltpu.roll(grad, pixels - 1, 1))
        elif col_tap == 2:
            shifted = jnp.where(place == 0, 0.0, pltpu.roll(grad, 1, 1))
        for row_tap in range(3):
            moved = shifted
            if row_tap == 0:
                moved = pltpu.roll(shifted, pixels - cols, 1) * lanes_ref[1:2, :]
            elif row_tap == 2:
                moved = pltpu.roll(shifted, cols, 1) * lanes_ref[0:1, :]
            tap = 3 * row_tap + col_tap
            columns_ref[tap * share : (tap + 1) * share, :] = moved.astype(jnp.bfloat16)
    part_ref[...] = jnp.dot(
        columns_ref[...], act_ref[...], preferred_element_type=jnp.float32
    ).astype(jnp.bfloat16)


def conv_back(grad_ref, weights_ref, ids_ref, taps_refs, total_ref, read, table_ref, which, cols):
    clear_edges(taps_refs, cols)
    mean, inverse, gain, shift = norm_rows(table_ref, which)
    sums = []

    def fill(rows):
        put_taps(taps_refs, grad_ref[rows, :].astype(jnp.float32), rows, cols)

    def slope(rows, value):
        normed = (read(rows) - mean) * inverse
        pre = normed * gain + shift
        part = smooth(pre)[1]
        grad = value * (part * (1.0 + pre * (1.0 - part)))
        sums.append((fold(grad), fold(grad * normed)))
        return grad

    run_conv(
        taps_refs, ids_ref, product_backward(weights_ref), total_ref, fill, slope, cols
    )
    return sum(pair[0] for pair in sums), sum(pair[1] for pair in sums)


def norm_back(total_ref, sums, read, table_ref, which):
    mean, inverse, gain, shift = norm_rows(table_ref, which)
    mean_grad, mean_cross = back_means(sums, gain, total_ref.shape[0])

    def back(rows):
        normed = (read(rows) - mean) * inverse
        return inverse * (total_ref[rows, :] * gain - mean_grad - normed * mean_cross)

    return back


def turn_kernel(
    ids_hbm, grad_ref, weights_ref, middle_ref, table_ref, total_ref, sums_ref, ids_ref, sem, *taps_refs, cols
):
    copy = pltpu.make_async_copy(ids_hbm, ids_ref, sem)
    copy.start()
    copy.wait()
    sums_ref[0:8, :], sums_ref[8:16, :] = conv_back(
        grad_ref,
        weights_ref.at[1],
        ids_ref,
        taps_refs,
        total_ref,
        lambda rows: middle_ref[rows, :],
        table_ref,
        1,
        cols,
    )


def norm_rows(table_ref, which):
    picks = (2 * which, 2 * which + 1, 6 + which, 9 + which)
    return tuple(table_ref[pick : pick + 1, :] for pick in picks)


def build_masks(ids_ref, lanes_ref, id_rows_ref, id_cols_ref, cols):
    rows = ids_ref.shape[1]
    for row in range(rows):
        here = ids_ref[0, row]
        place = slice(row * cols, (row + 1) * cols)
        id_rows_ref[place, :] = jnp.full((cols, LANES), here, jnp.int32)
    lane = lax.broadcasted_iota(jnp.int32, (8, LANES), 1)
    each = LANES // cols
    for block in range(rows // each):
        ids = jnp.full((8, LANES), ids_ref[0, block * each], jnp.int32)
        for step in range(1, each):
            ids = jnp.where(lane >= step * cols, ids_ref[0, block * each + step], ids)
        id_cols_ref[:, block * LANES : (block + 1) * LANES] = ids
    ids = id_cols_ref[...].astype(jnp.float32)
    pixels = ids.shape[1]
    pixel = lax.broadcasted_iota(jnp.int32, ids.shape, 1)
    above = jnp.where(pixel < cols, -1.0, pltpu.roll(ids, cols, 1))
    below = jnp.where(pixel >= pixels - cols, -1.0, pltpu.roll(ids, pixels - cols, 1))
    lanes_ref[0:1, :] = jnp.where(above == ids, 1.0, 0.0)[0:1]
    lanes_ref[1:2, :] = jnp.where(below == ids, 1.0, 0.0)[0:1]


def place_pieces(pieces, whole_ref, sems):
    own_pixels = whole_ref.shape[0] // len(pieces)
    height = lax.axis_index("height")
    copies = []
    for place, piece in enumerate(pieces):
        start = pl.multiple_of((height ^ place) * own_pixels, own_pixels)
        rows = pl.ds(start, own_pixels)
        copies.append(pltpu.make_async_copy(piece, whole_ref.at[rows, :], sems.at[place]))
    return copies


def conv_kernel(*refs, cols, count):
    pieces, refs = refs[:count], refs[count:]
    (
        ids_hbm,
        gains_hbm,
        shifts_hbm,
        biases_hbm,
        weights_hbm,
        qkv_hbm,
        proj_hbm,
        features_ref,
        act_one_ref,
        middle_ref,
        act_two_ref,
        residual_ref,
        table_ref,
        lanes_ref,
        id_rows_ref,
        id_cols_ref,
        turned_ref,
        qkv_ref,
        proj_ref,
        ids_ref,
        gains_ref,
        shifts_ref,
        biases_ref,
        weights_ref,
        own_ref,
        sems,
        piece_sem,
        *taps_refs,
    ) = refs
    pixels, channels = features_ref.shape
    wide = jnp.float32
    turned = [
        (
            weights_hbm.at[which, 2 - row_tap, 2 - col_tap],
            turned_ref.at[which, :, pl.ds((3 * row_tap + col_tap) * channels, channels)],
        )
        for which in (1, 0)
        for row_tap in range(3)
        for col_tap in range(3)
    ]
    moves = [
        (ids_hbm, ids_ref),
        (gains_hbm, gains_ref),
        (shifts_hbm, shifts_ref),
        (weights_hbm.at[0], weights_ref.at[0]),
        (biases_hbm, biases_ref),
        (weights_hbm.at[1], weights_ref.at[1]),
        (qkv_hbm, qkv_ref),
        (proj_hbm, proj_ref),
    ] + turned
    copies = [
        pltpu.make_async_copy(source, target, sems.at[index])
        for index, (source, target) in enumerate(moves)
    ]
    own_copy = pltpu.make_async_copy(pieces[0], own_ref, piece_sem)
    for copy in [own_copy] + copies[:6]:
        copy.start()
    clear_edges(taps_refs, cols)

    def read_input(rows):
        return features_ref[rows, :].astype(wide)

    def read_middle(rows):
        return middle_ref[rows, :]

    height = lax.axis_index("height")
    own_pixels = pixels // count
    seen = RunningStats()
    for place in list(range(1, count)) + [0]:
        if place == 0:
            own_copy.wait()
        piece = (pieces[place] if place else own_ref)[...]
        start = pl.multiple_of((height ^ place) * own_pixels, own_pixels)
        features_ref[pl.ds(start, own_pixels), :] = piece
        seen.add(piece.astype(wide))
    table_ref[0:1, :], table_ref[1:2, :] = seen.finish(pixels)
    copies[0].wait()
    build_masks(ids_ref, lanes_ref, id_rows_ref, id_cols_ref, cols)
    copies[1].wait()
    copies[2].wait()
    table_ref[6:9, :] = gains_ref[...]
    table_ref[9:12, :] = shifts_ref[...]
    for copy in copies[6:]:
        copy.start()
    copies[3].wait()
    copies[4].wait()
    seen = RunningStats()

    def keep(value):
        seen.add(value)
        return value

    run_conv(
        taps_refs,
        ids_ref,
        product_forward(weights_ref.at[0]),
        middle_ref,
        activation(read_input, *norm_rows(table_ref, 0), act_one_ref, taps_refs, cols),
        lambda rows, part: keep(part + biases_ref[0:1, :]),
        cols,
    )
    table_ref[2:3, :], table_ref[3:4, :] = seen.finish(pixels)
    copies[5].wait()
    seen = RunningStats()
    run_conv(
        taps_refs,
        ids_ref,
        product_forward(weights_ref.at[1]),
        residual_ref,
        activation(read_middle, *norm_rows(table_ref, 1), act_two_ref, taps_refs, cols),
        lambda rows, part: keep(part + (read_input(rows) + biases_ref[1:2, :])),
        cols,
    )
    table_ref[4:5, :], table_ref[5:6, :] = seen.finish(pixels)
    for copy in copies[6:]:
        copy.wait()


def score_kernel(
    qv_bias_hbm,
    proj_bias_hbm,
    qkv_ref,
    proj_ref,
    residual_ref,
    table_ref,
    id_rows_ref,
    id_cols_ref,
    normed_ref,
    query_ref,
    key_ref,
    value_ref,
    soft_ref,
    out_flip_ref,
    output_ref,
    qv_bias_ref,
    proj_bias_ref,
    value_flip_ref,
    sems,
    *,
    score_scale,
):
    pixels, channels = residual_ref.shape
    own_pixels = output_ref.shape[0]
    wide = jnp.float32
    exponent = score_scale * 1.4426950408889634
    moves = [(qv_bias_hbm, qv_bias_ref), (proj_bias_hbm, proj_bias_ref)]
    copies = [
        pltpu.make_async_copy(source, target, sems.at[index])
        for index, (source, target) in enumerate(moves)
    ]
    for copy in copies:
        copy.start()
    mean, inverse, gain, shift = norm_rows(table_ref, 2)
    scale = inverse * gain
    for copy in copies:
        copy.wait()
    block = min(QUERY_ROWS, pixels)

    def project(index, carry):
        rows = pl.ds(pl.multiple_of(index * block, block), block)
        normed = ((residual_ref[rows, :] - mean) * scale + shift).astype(jnp.bfloat16)
        normed_ref[rows, :] = normed
        query_ref[rows, :] = (
            jnp.dot(normed, qkv_ref[:, 0:channels], preferred_element_type=wide)
            + qv_bias_ref[0:1, :]
        ).astype(jnp.bfloat16)
        key_ref[rows, :] = jnp.dot(
            normed, qkv_ref[:, channels : 2 * channels], preferred_element_type=wide
        ).astype(jnp.bfloat16)
        values = (
            jnp.dot(normed, qkv_ref[:, 2 * channels :], preferred_element_type=wide)
            + qv_bias_ref[1:2, :]
        ).astype(jnp.bfloat16)
        value_ref[rows, :] = values
        value_flip_ref[:, rows] = values.T
        return carry

    lax.fori_loop(0, pixels // block, project, 0)

    def attend(index, carry):
        rows = pl.ds(pl.multiple_of(index * block, block), block)
        scores = lax.dot_general(
            key_ref[...], query_ref[rows, :], (((1,), (1,)), ((), ())), preferred_element_type=wide
        )
        same = widen(id_rows_ref[...], block) == id_cols_ref[0:1, rows]
        scores = jnp.where(same, scores, masked_score)
        scores = jnp.exp2((scores - jnp.max(scores, axis=0, keepdims=True)) * exponent)
        weights = scores * (1.0 / jnp.sum(scores, axis=0, keepdims=True))
        rounded = weights.astype(jnp.bfloat16)
        soft_ref[:, rows] = rounded
        out_flip_ref[:, rows] = jnp.dot(
            value_flip_ref[...], rounded, preferred_element_type=wide
        ).astype(jnp.bfloat16)
        return carry

    lax.fori_loop(0, pixels // block, attend, 0)
    height = lax.axis_index("height")
    own = pl.ds(pl.multiple_of(height * own_pixels, own_pixels), own_pixels)
    output_ref[...] = (
        residual_ref[own, :]
        + lax.dot_general(
            out_flip_ref[:, own],
            proj_ref[...],
            (((0,), (0,)), ((), ())),
            preferred_element_type=wide,
        )
        + proj_bias_ref[...]
    ).astype(jnp.bfloat16)


def own_quarter():
    height = lax.axis_index("height")
    return (height & 1) * 2 + ((height >> 1) & 1)


def send_order(source_ref, targets, axis, share):
    me = lax.axis_index("canvas")
    for step, target in enumerate(targets):
        place = pl.ds(pl.multiple_of((me ^ step) * share, share), share)
        target[...] = source_ref[place, :] if axis == 0 else source_ref[:, place]


def attention_kernel(
    proj_ref,
    normed_ref,
    query_ref,
    key_ref,
    value_ref,
    soft_ref,
    out_flip_ref,
    *refs,
    score_scale,
    count,
):
    pieces, (grad_ref, packed_ref, sums_ref), refs = (
        refs[:count],
        refs[count : count + 3],
        refs[count + 3 :],
    )
    *mixed_refs, mixed_ref, key_flip_ref, back_ref, score_grad_ref, flip_ref, sems = refs
    pixels, channels = normed_ref.shape
    block = min(QUERY_ROWS, pixels)
    wide = jnp.float32
    copies = place_pieces(pieces, grad_ref, sems)
    for copy in copies:
        copy.start()
    quarter = channels // 4
    own = pl.ds(pl.multiple_of(own_quarter() * quarter, quarter), quarter)
    flip_ref[...] = normed_ref[:, own].T
    key_flip_ref[...] = key_ref[...].T
    for copy in copies:
        copy.wait()

    for start in range(0, pixels, block):
        rows = slice(start, start + block)
        back_ref[rows, :] = lax.dot_general(
            grad_ref[rows, :], proj_ref[...], (((1,), (1,)), ((), ())), preferred_element_type=wide
        ).astype(jnp.bfloat16)
    for start in range(0, pixels, block):
        rows = slice(start, start + block)
        weights = soft_ref[:, rows].astype(wide)
        weight_grad = lax.dot_general(
            value_ref[...],
            back_ref[rows, :],
            (((1,), (1,)), ((), ())),
            preferred_element_type=wide,
        )
        dots = jnp.sum(weights * weight_grad, axis=0, keepdims=True)
        score_grad = (weights * (weight_grad - dots)).astype(jnp.bfloat16)
        score_grad_ref[:, rows] = score_grad
        query_grad = jnp.dot(key_flip_ref[...], score_grad, preferred_element_type=wide)
        packed_ref[rows, 0:channels] = (query_grad * score_scale).astype(jnp.bfloat16).T
        packed_ref[rows, 2 * channels :] = jnp.dot(
            soft_ref[rows, :], back_ref[...], preferred_element_type=wide
        ).astype(jnp.bfloat16)
    for start in range(0, pixels, block):
        rows = slice(start, start + block)
        packed_ref[rows, channels : 2 * channels] = (
            jnp.dot(score_grad_ref[rows, :], query_ref[...], preferred_element_type=wide)
            * score_scale
        ).astype(jnp.bfloat16)

    def pack(rows, carry):
        return (
            carry[0] + fold(packed_ref[rows, 0:channels].astype(wide)),
            carry[1] + fold(packed_ref[rows, 2 * channels :].astype(wide)),
            carry[2] + fold(grad_ref[rows, :].astype(wide)),
        )

    zeros = jnp.zeros((8, channels), wide)
    totals = zeros, zeros, zeros
    for start in range(0, pixels, CHUNK):
        totals = pack(pl.ds(start, CHUNK), totals)
    sums_ref[...] = jnp.zeros(sums_ref.shape, wide)
    for row, total in enumerate(totals):
        sums_ref[8 + row : 9 + row, :] = column_total(total)
    mixed_ref[:, 0 : 3 * channels] = jnp.dot(
        flip_ref[...], packed_ref[...], preferred_element_type=wide
    ).astype(jnp.bfloat16)
    mixed_ref[:, 3 * channels :] = jnp.dot(
        out_flip_ref[own, :], grad_ref[...], preferred_element_type=wide
    ).astype(jnp.bfloat16)
    send_order(mixed_ref, mixed_refs, 0, quarter // len(mixed_refs))


def third_kernel(
    qkv_ref,
    grad_ref,
    packed_ref,
    residual_ref,
    table_ref,
    act_two_ref,
    lanes_ref,
    old_sums_ref,
    residual_grad_ref,
    grad_two_ref,
    sums_ref,
    part_ref,
    total_ref,
    flip_ref,
    columns_ref,
    *,
    cols,
):
    pixels, channels = residual_ref.shape
    block = pixels
    wide = jnp.float32
    mean, inverse, gain, shift = norm_rows(table_ref, 2)
    zeros = jnp.zeros((8, channels), wide)

    sums = (zeros, zeros)
    for start in range(0, pixels, block):
        rows = pl.ds(start, block)
        normed_grad = lax.dot_general(
            packed_ref[rows, :], qkv_ref[...], (((1,), (1,)), ((), ())), preferred_element_type=wide
        )
        total_ref[rows, :] = normed_grad
        normed = (residual_ref[rows, :] - mean) * inverse
        sums = sums[0] + fold(normed_grad), sums[1] + fold(normed_grad * normed)
    sums_ref[...] = old_sums_ref[...]
    sums_ref[5:6, :] = column_total(sums[1])
    sums_ref[6:7, :] = column_total(sums[0])
    mean_grad, mean_cross = back_means(sums, gain, pixels)

    def finish(rows, carry):
        normed = (residual_ref[rows, :] - mean) * inverse
        back = inverse * (total_ref[rows, :] * gain - mean_grad - normed * mean_cross)
        total = grad_ref[rows, :].astype(wide) + back
        residual_grad_ref[rows, :] = total
        low = total.astype(jnp.bfloat16)
        grad_two_ref[rows, :] = low
        return carry + fold(low.astype(wide))

    sums_ref[7:8, :] = column_total(each_chunk(pixels, finish, zeros))
    weight_part(act_two_ref, grad_two_ref, lanes_ref, flip_ref, columns_ref, part_ref, cols)


def second_kernel(
    total_ref,
    partial_ref,
    middle_ref,
    table_ref,
    act_one_ref,
    lanes_ref,
    old_sums_ref,
    part_two_ref,
    grad_one_ref,
    sums_ref,
    keep_one_ref,
    send_one_ref,
    keep_two_ref,
    send_two_ref,
    flip_ref,
    columns_ref,
    part_ref,
    *,
    cols,
):
    pixels, channels = middle_ref.shape
    sums = partial_ref[0:8, :], partial_ref[8:16, :]
    back = norm_back(total_ref, sums, lambda rows: middle_ref[rows, :], table_ref, 1)
    sums_ref[...] = old_sums_ref[...]
    sums_ref[2:3, :] = column_total(sums[1])
    sums_ref[3:4, :] = column_total(sums[0])

    def finish(rows, carry):
        low = back(rows).astype(jnp.bfloat16)
        grad_one_ref[rows, :] = low
        return carry + fold(low.astype(jnp.float32))

    zeros = jnp.zeros((8, channels), jnp.float32)
    sums_ref[4:5, :] = column_total(each_chunk(pixels, finish, zeros))
    weight_part(act_one_ref, grad_one_ref, lanes_ref, flip_ref, columns_ref, part_ref, cols)
    me = lax.axis_index("canvas")
    rows = part_ref.shape[0]
    for source_ref, near, far, keep_ref, send_ref in (
        (part_ref, 1, 2, keep_one_ref, send_one_ref),
        (part_two_ref, 2, 1, keep_two_ref, send_two_ref),
    ):
        width = keep_ref.shape[1]
        for target_ref, flip in ((keep_ref, 0), (send_ref, near)):
            for slot in range(2):
                owner = me ^ flip ^ (slot * far)
                place = pl.ds(pl.multiple_of(owner * width, width), width)
                target_ref[slot * rows : (slot + 1) * rows, :] = source_ref[:, place]


def first_kernel(
    ids_hbm,
    grad_one_ref,
    features_ref,
    residual_grad_ref,
    table_ref,
    old_sums_ref,
    weights_ref,
    input_grad_ref,
    sums_ref,
    total_ref,
    ids_ref,
    sem,
    *taps_refs,
    cols,
):
    copy = pltpu.make_async_copy(ids_hbm, ids_ref, sem)
    copy.start()
    copy.wait()

    def read(rows):
        return features_ref[rows, :].astype(jnp.float32)

    sums = conv_back(
        grad_one_ref, weights_ref.at[0], ids_ref, taps_refs, total_ref, read, table_ref, 0, cols
    )
    back = norm_back(total_ref, sums, read, table_ref, 0)
    sums_ref[...] = old_sums_ref[...]
    sums_ref[0:1, :] = column_total(sums[1])
    sums_ref[1:2, :] = column_total(sums[0])
    count = input_grad_ref.shape[0]
    own = pl.ds(pl.multiple_of(lax.axis_index("height") * count, count), count)
    input_grad_ref[...] = (residual_grad_ref[own, :] + back(own)).astype(jnp.bfloat16)


def place_kernel(*refs):
    joints, (qkv_hbm, proj_hbm, packed_ref, qkv_ref, proj_ref, sems) = refs[:-6], refs[-6:]
    share = packed_ref.shape[0] // len(joints)
    me = lax.axis_index("canvas")
    for step, joint in enumerate(joints):
        place = pl.ds(pl.multiple_of((me ^ step) * share, share), share)
        packed_ref[place, :] = joint[...]
    spread_quarters([packed_ref], 0, qkv_ref, proj_ref, qkv_hbm, proj_hbm, sems)


def spread_quarters(packed, offset, qkv_ref, proj_ref, qkv_hbm, proj_hbm, sems):
    quarter = packed[0].shape[0]
    inner = qkv_ref.shape[2]
    copies = []
    for index, packed_ref in enumerate(packed):
        owner = own_quarter() ^ (index + offset)
        rows = pl.ds(pl.multiple_of(owner * quarter, quarter), quarter)
        qkv_ref[index] = packed_ref[:, 0:inner].astype(jnp.float32)
        proj_ref[index] = packed_ref[:, inner:].astype(jnp.float32)
        for which, (held, target) in enumerate(((qkv_ref, qkv_hbm), (proj_ref, proj_hbm))):
            copy = pltpu.make_async_copy(held.at[index], target.at[rows, :], sems.at[index, which])
            copy.start()
            copies.append(copy)
    for copy in copies:
        copy.wait()


def join_kernel(*refs):
    ins, (qkv_hbm, proj_hbm, qkv_ref, proj_ref, sems) = refs[:-5], refs[-5:]
    packed = ins[2:]
    spread_quarters(packed, 1, qkv_ref, proj_ref, qkv_hbm, proj_hbm, sems)


def halve_kernel(
    keep_one_ref,
    got_one_ref,
    keep_two_ref,
    got_two_ref,
    hold_one_ref,
    send_one_ref,
    hold_two_ref,
    send_two_ref,
):
    for keep_ref, got_ref, hold_ref, send_ref in (
        (keep_one_ref, got_one_ref, hold_one_ref, send_one_ref),
        (keep_two_ref, got_two_ref, hold_two_ref, send_two_ref),
    ):
        total = keep_ref[...].astype(jnp.float32) + got_ref[...].astype(jnp.float32)
        rows = hold_ref.shape[0]
        hold_ref[...] = total[0:rows]
        send_ref[...] = total[rows:].astype(jnp.bfloat16)


def sums_kernel(
    sums_ref,
    got_sums_ref,
    hold_one_ref,
    got_one_ref,
    hold_two_ref,
    got_two_ref,
    share_ref,
    gains_ref,
    shifts_ref,
    conv_ref,
    qv_ref,
    proj_ref,
):
    for which, (hold_ref, got_ref) in enumerate(
        ((hold_one_ref, got_one_ref), (hold_two_ref, got_two_ref))
    ):
        total = hold_ref[...] + got_ref[...].astype(jnp.float32)
        share_ref[which] = total.reshape(share_ref.shape[1:])
    total = sums_ref[...] + got_sums_ref[...]
    for row, start in enumerate((0, 2, 5)):
        gains_ref[row : row + 1, :] = total[start : start + 1]
        shifts_ref[row : row + 1, :] = total[start + 1 : start + 2]
    conv_ref[0:1, :] = total[4:5]
    conv_ref[1:2, :] = total[7:8]
    qv_ref[...] = total[8:10]
    proj_ref[...] = total[10:11]


def call_kernel(kernel, outputs, scratch, operands, places, flops, limit, out_places=None, aliases={}):
    out_places = out_places or "v" * len(outputs)
    spaces = {
        "v": pl.BlockSpec(memory_space=pltpu.VMEM),
        "s": pl.BlockSpec(memory_space=pltpu.SMEM),
        "h": pl.BlockSpec(memory_space=pl.ANY),
        "o": pl.BlockSpec(memory_space=pltpu.VMEM),
        "a": pl.BlockSpec(memory_space=pl.ANY),
    }
    moved = 8 * flops // LANES
    held = {"v": pltpu.VMEM, "h": pltpu.HBM, "o": jax.ShapeDtypeStruct}
    operands = [
        pltpu.with_memory_space_constraint(array, pltpu.HBM) if place == "h" else array
        for array, place in zip(operands, places)
    ]
    return pl.pallas_call(
        kernel,
        out_shape=[held[place](*output) for output, place in zip(outputs, out_places)],
        in_specs=[spaces[place] for place in places],
        out_specs=[spaces[place] for place in out_places],
        scratch_shapes=scratch,
        input_output_aliases=aliases,
        compiler_params=pltpu.CompilerParams(vmem_limit_bytes=limit * 2**20),
        cost_estimate=pl.CostEstimate(flops=flops, bytes_accessed=moved, transcendentals=0),
    )(*operands)


def send_height(block, step):
    size = lax.axis_size("height")
    return lax.ppermute(block, "height", [(i, i ^ step) for i in range(size)])


def with_cores(blocks):
    return [piece for block in blocks for piece in (block, send_height(block, 1))]


def send_canvas(block, step):
    size = lax.axis_size("canvas")
    return lax.ppermute(block, "canvas", [(i, i ^ step) for i in range(size)])


def trade_canvas(pieces):
    return [pieces[0]] + [send_canvas(piece, step) for step, piece in enumerate(pieces) if step]


def whole_canvas(
    features,
    tile_ids,
    norm_gains,
    norm_shifts,
    conv_weights,
    conv_biases,
    qkv_weight,
    qv_bias,
    proj_weight,
    proj_bias,
    cotangent,
):
    height_size = lax.axis_size("height")
    canvas_size = lax.axis_size("canvas")
    local_rows, cols, channels = features.shape[1:]
    all_rows = tile_ids.shape[1]
    pixels = all_rows * cols
    own_pixels = local_rows * cols
    out_share = channels // height_size
    ci_share = channels // canvas_size
    quarter = channels // 4
    row_share = quarter // canvas_size
    low, wide = jnp.bfloat16, jnp.float32

    own_features = features.reshape(own_pixels, channels)
    own_grad = cotangent.reshape(own_pixels, channels)
    steps = range(2, height_size, 2)
    held_features = [own_features] + [send_height(own_features, step) for step in steps]
    pieces = with_cores(held_features)
    near_grad, pieces[2] = lax.optimization_barrier((own_grad, held_features[1]))
    far_grad, *pieces[4::2] = lax.optimization_barrier((own_grad, *held_features[2:]))
    held_grads = [own_grad, send_height(near_grad, 2)]
    held_grads += [send_height(far_grad, step) for step in steps[1:]]

    plane = ((pixels, channels), low)
    plane_wide = ((pixels, channels), wide)
    sums_shape = ((16, channels), wide)
    mixed_shapes = [((row_share, 4 * channels), low)] * canvas_size
    taps = [pltpu.VMEM((cols + CONV_ROWS, 3 * channels), low)] * (pixels // CONV_ROWS)
    held_ids = pltpu.SMEM(tile_ids.shape, jnp.int32)
    held_wide = pltpu.VMEM((pixels, channels), wide)
    flipped = pltpu.VMEM((channels, pixels), low)
    narrow = pltpu.VMEM((NARROW, pixels), low)
    columns = pltpu.VMEM((9 * out_share, pixels), low)
    part_held = pltpu.VMEM((9 * out_share, channels), low)
    sem = pltpu.SemaphoreType.DMA
    conv_flops = 2 * 9 * pixels * channels * channels
    dot_flops = 2 * pixels * channels * channels
    score_flops = 2 * pixels * pixels * channels
    scale = channels ** (-0.5)

    (
        all_features,
        act_one,
        middle,
        act_two,
        residual,
        table,
        lane_mask,
        id_rows,
        id_cols,
        turned,
        held_qkv,
        held_proj,
    ) = call_kernel(
        functools.partial(conv_kernel, cols=cols, count=height_size),
        [
            plane,
            plane,
            plane_wide,
            plane,
            plane_wide,
            ((16, channels), wide),
            ((8, pixels), wide),
            ((pixels, LANES), jnp.int32),
            ((8, pixels), jnp.int32),
            ((2, channels, 9 * channels), low),
            (qkv_weight.shape, low),
            (proj_weight.shape, low),
        ],
        [
            held_ids,
            pltpu.VMEM(norm_gains.shape, wide),
            pltpu.VMEM(norm_shifts.shape, wide),
            pltpu.VMEM(conv_biases.shape, wide),
            pltpu.VMEM(conv_weights.shape, low),
            pltpu.VMEM((own_pixels, channels), low),
            sem((26,)),
            sem,
            *taps,
        ],
        [
            *pieces,
            tile_ids,
            norm_gains,
            norm_shifts,
            conv_biases,
            conv_weights,
            qkv_weight,
            proj_weight,
        ],
        "h" + "v" * (height_size - 1) + "h" * 7,
        2 * conv_flops,
        24,
    )
    residual, *held_grads = lax.optimization_barrier((residual, *held_grads))
    grad_pieces = with_cores(held_grads)
    normed, query, key, value, soft, out_flip, output = call_kernel(
        functools.partial(score_kernel, score_scale=scale),
        [
            plane,
            plane,
            plane,
            plane,
            ((pixels, pixels), low),
            ((channels, pixels), low),
            ((own_pixels, channels), low),
        ],
        [
            pltpu.VMEM(qv_bias.shape, wide),
            pltpu.VMEM((1, channels), wide),
            flipped,
            sem((2,)),
        ],
        [
            qv_bias,
            proj_bias.reshape(1, channels),
            held_qkv,
            held_proj,
            residual,
            table,
            id_rows,
            id_cols,
        ],
        "hhvvvvvv",
        3 * dot_flops + 2 * score_flops,
        16,
        "v" * 6 + "o",
    )
    normed, *grad_pieces = lax.optimization_barrier((normed, *grad_pieces))
    all_grad, packed, sums, *mixed = call_kernel(
        functools.partial(attention_kernel, score_scale=scale, count=height_size),
        [plane, ((pixels, 3 * channels), low), sums_shape, *mixed_shapes],
        [
            pltpu.VMEM((quarter, 4 * channels), low),
            flipped,
            pltpu.VMEM((pixels, channels), low),
            pltpu.VMEM((pixels, pixels), low),
            pltpu.VMEM((quarter, pixels), low),
            sem((height_size,)),
        ],
        [held_proj, normed, query, key, value, soft, out_flip, *grad_pieces],
        "vvvvvvvh" + "a" * (height_size - 1),
        3 * dot_flops + 4 * score_flops,
        20,
    )
    mixed = trade_canvas(mixed)
    residual_grad, grad_two, sums, part_two = call_kernel(
        functools.partial(third_kernel, cols=cols),
        [plane_wide, plane, sums_shape, ((9 * out_share, channels), low)],
        [held_wide, narrow, columns],
        [held_qkv, all_grad, packed, residual, table, act_two, lane_mask, sums],
        "vvvvvvvv",
        3 * dot_flops + conv_flops // height_size,
        16,
    )
    grad_two, *mixed = lax.optimization_barrier((grad_two, *mixed))
    mixed_sum = mixed[0].astype(wide)
    for piece in mixed[1:]:
        mixed_sum = mixed_sum + piece.astype(wide)
    joints = trade_canvas([mixed_sum.astype(low)] * canvas_size)
    act_two_grad, partial_sums = call_kernel(
        functools.partial(turn_kernel, cols=cols),
        [plane_wide, sums_shape],
        [held_ids, sem, *taps],
        [tile_ids, grad_two, turned, middle, table],
        "hvvvv",
        conv_flops,
        16,
    )
    act_two_grad, *joints = lax.optimization_barrier((act_two_grad, *joints))
    qkv_grad, proj_grad, own_mixed = call_kernel(
        place_kernel,
        [(qkv_weight.shape, wide), (proj_weight.shape, wide), ((quarter, 4 * channels), low)],
        [
            pltpu.VMEM((1, quarter, 3 * channels), wide),
            pltpu.VMEM((1, quarter, channels), wide),
            sem((1, 2)),
        ],
        joints,
        "v" * canvas_size,
        0,
        12,
        "hhv",
    )
    chip_mixed = send_height(own_mixed, 2)
    core_mixed = send_height(own_mixed, 1)
    grad_one, sums, keep_one, send_one, keep_two, send_two = call_kernel(
        functools.partial(second_kernel, cols=cols),
        [plane, sums_shape] + [((18 * out_share, ci_share), low)] * 4,
        [narrow, columns, part_held],
        [act_two_grad, partial_sums, middle, table, act_one, lane_mask, sums, part_two],
        "vvvvvvvv",
        conv_flops // height_size,
        16,
    )
    got_one, got_two = send_canvas(send_one, 1), send_canvas(send_two, 2)
    input_grad, sums = call_kernel(
        functools.partial(first_kernel, cols=cols),
        [((own_pixels, channels), low), sums_shape],
        [held_wide, held_ids, sem, *taps],
        [tile_ids, grad_one, all_features, residual_grad, table, sums, turned],
        "hvvvvvv",
        0,
        16,
        "ov",
    )
    sums, chip_mixed, core_mixed, got_one, got_two = lax.optimization_barrier(
        (sums, chip_mixed, core_mixed, got_one, got_two)
    )
    got_sums = send_canvas(sums, 1)
    got_sums, keep_one = lax.optimization_barrier((got_sums, keep_one))
    hold_one, send_one, hold_two, send_two = call_kernel(
        halve_kernel,
        [((9 * out_share, ci_share), kind) for kind in (wide, low, wide, low)],
        [],
        [keep_one, got_one, keep_two, got_two],
        "vvvv",
        0,
        12,
    )
    got_one, got_two = send_canvas(send_one, 2), send_canvas(send_two, 1)
    both_mixed = send_height(chip_mixed, 1)
    sums = sums + got_sums
    got_sums = send_canvas(sums, 2)
    qkv_grad, proj_grad = call_kernel(
        join_kernel,
        [(qkv_weight.shape, wide), (proj_weight.shape, wide)],
        [
            pltpu.VMEM((3, quarter, 3 * channels), wide),
            pltpu.VMEM((3, quarter, channels), wide),
            sem((3, 2)),
        ],
        [qkv_grad, proj_grad, chip_mixed, core_mixed, both_mixed],
        "hhvvv",
        0,
        12,
        "hh",
        {0: 0, 1: 1},
    )
    qkv_grad, got_sums, got_one, got_two = lax.optimization_barrier(
        (qkv_grad, got_sums, got_one, got_two)
    )
    vector_shapes = [norm_gains.shape, norm_shifts.shape, conv_biases.shape, qv_bias.shape]
    conv_grad, gains_grad, shifts_grad, biases_grad, qv_grad, proj_bias_grad = call_kernel(
        sums_kernel,
        [((2, 3, 3, out_share, ci_share), wide)]
        + [(shape, wide) for shape in vector_shapes + [(1, channels)]],
        [],
        [sums, got_sums, hold_one, got_one, hold_two, got_two],
        "vvvvvv",
        0,
        12,
        "o" * 6,
    )
    own_shape = (1, local_rows, cols, channels)
    return (
        output.reshape(own_shape),
        input_grad.reshape(own_shape),
        gains_grad,
        shifts_grad,
        jnp.swapaxes(conv_grad, 3, 4),
        biases_grad,
        qkv_grad,
        qv_grad,
        proj_grad,
        proj_bias_grad.reshape(channels),
    )


def on_device(*arrays):
    features, tile_ids = arrays[0], arrays[1]
    local_rows, cols, channels = features.shape[1:]
    pixels = tile_ids.shape[1] * cols
    height_size, canvas_size = lax.axis_size("height"), lax.axis_size("canvas")
    powers = all(size & (size - 1) == 0 for size in (height_size, canvas_size, cols))
    fits = (
        powers
        and height_size > 2
        and canvas_size == 4
        and channels == LANES * canvas_size
        and pixels <= MOST_PIXELS
        and pixels % CONV_ROWS == 0
        and CONV_ROWS % CHUNK == 0
        and (local_rows * cols) % LANES == 0
        and CHUNK % cols == 0
        and cols % 16 == 0
        and channels % (LANES * canvas_size) == 0
        and 2 * channels == NARROW * height_size
    )
    return whole_canvas(*arrays) if fits else split_canvas(*arrays)


def solution(mesh):
    in_specs = (
        P("canvas", "height", None, None),
        P("canvas", None),
        P(),
        P(),
        P(),
        P(),
        P(),
        P(),
        P(),
        P(),
        P("canvas", "height", None, None),
    )
    out_specs = (
        P("canvas", "height", None, None),
        P("canvas", "height", None, None),
        P(),
        P(),
        P(None, None, None, "canvas", "height"),
        P(),
        P(),
        P(),
        P(),
        P(),
    )
    return jax.shard_map(
        on_device, mesh=mesh, in_specs=in_specs, out_specs=out_specs, check_vma=False
    )
```

```python
import functools

import jax
import jax.numpy as jnp
from jax import lax
from jax.experimental import pallas as pl
from jax.experimental.pallas import tpu as pltpu
from jax.sharding import PartitionSpec as P

GROUPS = 32


epsilon = 1e-06
masked_score = -1e30
MOST_PIXELS = 1024
LANES = 128
NARROW = 128
CHUNK = 128
CONV_ROWS = 1024
FILL_ROWS = 256
QUERY_ROWS = 512
KEY_ROWS = 256


def extended(block, sides, width):
    for axis, dim in sides:
        count = lax.axis_size(axis)
        forward = [(i, i + 1) for i in range(count - 1)]
        backward = [(target, source) for source, target in forward]
        low = lax.ppermute(
            lax.slice_in_dim(block, block.shape[dim] - width, None, axis=dim), axis, forward
        )
        high = lax.ppermute(lax.slice_in_dim(block, 0, width, axis=dim), axis, backward)
        block = jnp.concatenate([low, block, high], axis=dim)
    return block


def group_total(vector):
    return vector.reshape(GROUPS, -1).sum(axis=1)


def spread_groups(vector, channels):
    return jnp.repeat(vector, channels // GROUPS)


def norm_forward(values, gain, shift, members):
    channels = values.shape[1]
    totals = lax.psum(group_total(jnp.sum(values, axis=0)), "height")
    centered = values - spread_groups(totals / members, channels)
    squares = lax.psum(group_total(jnp.sum(centered * centered, axis=0)), "height")
    inverse = spread_groups(lax.rsqrt(squares / members + epsilon), channels)
    normed = centered * inverse
    return (normed, inverse, normed * gain + shift)


def norm_backward(grad_in, normed, inverse, gain, members):
    channels = grad_in.shape[1]
    scaled = grad_in * gain
    both_sums = lax.psum(
        (group_total(jnp.sum(scaled, axis=0)), group_total(jnp.sum(scaled * normed, axis=0))),
        "height",
    )
    mean_grad = spread_groups(both_sums[0] / members, channels)
    mean_cross = spread_groups(both_sums[1] / members, channels)
    result = inverse * (scaled - mean_grad - normed * mean_cross)
    return (result, jnp.sum(grad_in * normed, axis=0), jnp.sum(grad_in, axis=0))


def swish(values):
    return values * jax.nn.sigmoid(values)


def swish_slope(values):
    sigmoid_part = jax.nn.sigmoid(values)
    return sigmoid_part * (1.0 + values * (1.0 - sigmoid_part))


def tap_columns(padded, row_mask, local_rows, canvas_cols):
    pieces = []
    for row_tap in range(3):
        rows_taken = padded[row_tap : row_tap + local_rows] * row_mask[:, row_tap, None, None]
        for col_tap in range(3):
            pieces.append(rows_taken[:, col_tap : col_tap + canvas_cols])
    stacked = jnp.concatenate(pieces, axis=2)
    return stacked.reshape(local_rows * canvas_cols, stacked.shape[2])


def conv_forward(acts, row_mask, weight, bias):
    local_rows, canvas_cols, channels = acts.shape
    rimmed = extended(acts, (("height", 0),), 1)
    padded = jnp.pad(rimmed, ((0, 0), (1, 1), (0, 0)))
    gathered = tap_columns(padded, row_mask, local_rows, canvas_cols)
    result = (
        jnp.dot(
            gathered, weight.reshape(9 * channels, channels), preferred_element_type=jnp.float32
        )
        + bias
    )
    return (result, gathered)


def conv_backward(grad_low, row_mask, weight, gathered):
    local_rows, canvas_cols, channels = grad_low.shape
    flat_grad = grad_low.reshape(local_rows * canvas_cols, channels)
    weight_grad = lax.dot_general(
        gathered, flat_grad, (((0,), (0,)), ((), ())), preferred_element_type=jnp.float32
    )
    rimmed = extended(grad_low, (("height", 0),), 1)
    padded = jnp.pad(rimmed, ((0, 0), (1, 1), (0, 0)))
    grad_taps = tap_columns(padded, row_mask, local_rows, canvas_cols)
    flipped = jnp.transpose(weight[::-1, ::-1], (0, 1, 3, 2)).reshape(9 * channels, channels)
    input_part = jnp.dot(grad_taps, flipped, preferred_element_type=jnp.float32)
    return (
        input_part,
        weight_grad.reshape(3, 3, channels, channels),
        jnp.sum(flat_grad.astype(jnp.float32), axis=0),
    )


def take_rows(array, offset, count):
    return lax.dynamic_slice_in_dim(array, offset, count)


def score_grads(
    queries, out_grad, log_total, row_dots, query_ids, key_rows, value_rows, key_ids, score_scale
):
    scores = (
        lax.dot_general(
            queries, key_rows, (((1,), (1,)), ((), ())), preferred_element_type=jnp.float32
        )
        * score_scale
    )
    same_tile = query_ids[:, None] == key_ids[None, :]
    softmax_block = jnp.exp(jnp.where(same_tile, scores - log_total[:, None], masked_score))
    weight_grad = lax.dot_general(
        out_grad, value_rows, (((1,), (1,)), ((), ())), preferred_element_type=jnp.float32
    )
    score_grad = (softmax_block * (weight_grad - row_dots[:, None])).astype(jnp.bfloat16)
    return (softmax_block.astype(jnp.bfloat16), score_grad)


def split_canvas(
    features,
    tile_ids,
    norm_gains,
    norm_shifts,
    conv_weights,
    conv_biases,
    qkv_weight,
    qv_bias,
    proj_weight,
    proj_bias,
    cotangent,
):
    height_size = lax.axis_size("height")
    local_rows = features.shape[1]
    canvas_cols = features.shape[2]
    channels = features.shape[3]
    pixels = local_rows * canvas_cols
    row_ids = tile_ids[0]
    all_rows = row_ids.shape[0]
    members = float(all_rows * canvas_cols * (channels // GROUPS))
    score_scale = channels ** (-0.5)
    first_row = lax.axis_index("height") * local_rows
    edge_ids = jnp.full((1,), -1, jnp.int32)
    padded_ids = jnp.concatenate([edge_ids, row_ids, edge_ids])
    near_ids = lax.dynamic_slice_in_dim(padded_ids, first_row, local_rows + 2)
    own_rows = near_ids[1 : local_rows + 1]
    row_mask = jnp.stack(
        [near_ids[row_tap : row_tap + local_rows] == own_rows for row_tap in range(3)], axis=1
    ).astype(jnp.bfloat16)
    key_ids = jnp.repeat(row_ids, canvas_cols)
    query_ids = jnp.repeat(own_rows, canvas_cols)
    grid_shape = (local_rows, canvas_cols, channels)
    inputs = features[0].reshape(pixels, channels).astype(jnp.float32)
    normed_one, inverse_one, pre_one = norm_forward(inputs, norm_gains[0], norm_shifts[0], members)
    act_one = swish(pre_one).astype(jnp.bfloat16).reshape(grid_shape)
    middle, taps_one = conv_forward(act_one, row_mask, conv_weights[0], conv_biases[0])
    normed_two, inverse_two, pre_two = norm_forward(middle, norm_gains[1], norm_shifts[1], members)
    act_two = swish(pre_two).astype(jnp.bfloat16).reshape(grid_shape)
    branch, taps_two = conv_forward(act_two, row_mask, conv_weights[1], conv_biases[1])
    residual = inputs + branch
    normed_three, inverse_three, pre_three = norm_forward(
        residual, norm_gains[2], norm_shifts[2], members
    )
    attn_input = pre_three.astype(jnp.bfloat16)
    mixed = jnp.dot(attn_input, qkv_weight, preferred_element_type=jnp.float32)
    queries = (mixed[:, :channels] + qv_bias[0]).astype(jnp.bfloat16)
    key_rows = mixed[:, channels : 2 * channels].astype(jnp.bfloat16)
    value_rows = (mixed[:, 2 * channels :] + qv_bias[1]).astype(jnp.bfloat16)
    running_max = jnp.full((pixels,), masked_score, jnp.float32)
    key_piece = lax.all_gather(key_rows, "height", axis=0, tiled=True)
    value_piece = lax.all_gather(value_rows, "height", axis=0, tiled=True)
    scores = (
        lax.dot_general(
            queries, key_piece, (((1,), (1,)), ((), ())), preferred_element_type=jnp.float32
        )
        * score_scale
    )
    same_tile = query_ids[:, None] == key_ids[None, :]
    scores = jnp.where(same_tile, scores, masked_score)
    new_max = jnp.maximum(running_max, jnp.max(scores, axis=1))
    weights = jnp.where(same_tile, jnp.exp(scores - new_max[:, None]), 0.0)
    summed_out = jnp.dot(
        weights.astype(jnp.bfloat16), value_piece, preferred_element_type=jnp.float32
    )
    total_weight = jnp.sum(weights, axis=1)
    log_total = new_max + jnp.log(total_weight)
    attended = summed_out / total_weight[:, None]
    attended_low = attended.astype(jnp.bfloat16)
    output = (
        residual
        + jnp.dot(attended_low, proj_weight, preferred_element_type=jnp.float32)
        + proj_bias
    )
    out_grad = cotangent[0].reshape(pixels, channels)
    out_grad_full = out_grad.astype(jnp.float32)
    proj_grad = lax.dot_general(
        attended_low, out_grad, (((0,), (0,)), ((), ())), preferred_element_type=jnp.float32
    )
    proj_bias_grad = jnp.sum(out_grad_full, axis=0)
    attended_grad = lax.dot_general(
        out_grad, proj_weight, (((1,), (1,)), ((), ())), preferred_element_type=jnp.float32
    ).astype(jnp.bfloat16)
    row_dots = jnp.sum(attended_grad.astype(jnp.float32) * attended, axis=1)
    block_rows = pixels * min(height_size, 8)
    zero_block = jnp.zeros((pixels, channels), jnp.float32)
    key_all, value_all = (
        lax.all_gather(key_rows, "height", axis=0, tiled=True),
        lax.all_gather(value_rows, "height", axis=0, tiled=True),
    )
    query_all, grad_all = (
        lax.all_gather(queries, "height", axis=0, tiled=True),
        lax.all_gather(attended_grad, "height", axis=0, tiled=True),
    )
    total_all, dots_all = (
        lax.all_gather(log_total, "height", axis=0, tiled=True),
        lax.all_gather(row_dots, "height", axis=0, tiled=True),
    )

    def own_query_step(running, block_index):
        offset = block_index * block_rows
        key_part = take_rows(key_all, offset, block_rows)
        rounded, score_grad = score_grads(
            queries,
            attended_grad,
            log_total,
            row_dots,
            query_ids,
            key_part,
            take_rows(value_all, offset, block_rows),
            take_rows(key_ids, offset, block_rows),
            score_scale,
        )
        return (
            running
            + jnp.dot(score_grad, key_part, preferred_element_type=jnp.float32) * score_scale,
            None,
        )

    def own_key_step(running, block_index):
        offset = block_index * block_rows
        query_part = take_rows(query_all, offset, block_rows)
        grad_part = take_rows(grad_all, offset, block_rows)
        rounded, score_grad = score_grads(
            query_part,
            grad_part,
            take_rows(total_all, offset, block_rows),
            take_rows(dots_all, offset, block_rows),
            take_rows(key_ids, offset, block_rows),
            key_rows,
            value_rows,
            query_ids,
            score_scale,
        )
        key_part = (
            lax.dot_general(
                score_grad, query_part, (((0,), (0,)), ((), ())), preferred_element_type=jnp.float32
            )
            * score_scale
        )
        value_part = lax.dot_general(
            rounded, grad_part, (((0,), (0,)), ((), ())), preferred_element_type=jnp.float32
        )
        return ((running[0] + key_part, running[1] + value_part), None)

    block_count = key_all.shape[0] // block_rows
    query_grad, unused_one = lax.scan(own_query_step, zero_block, jnp.arange(block_count))
    (key_grad, value_grad), unused_two = lax.scan(
        own_key_step, (zero_block, zero_block), jnp.arange(block_count)
    )
    query_low = query_grad.astype(jnp.bfloat16)
    key_low = key_grad.astype(jnp.bfloat16)
    value_low = value_grad.astype(jnp.bfloat16)
    stacked_grad = jnp.concatenate([query_low, key_low, value_low], axis=1)
    qkv_grad = lax.dot_general(
        attn_input, stacked_grad, (((0,), (0,)), ((), ())), preferred_element_type=jnp.float32
    )
    qv_grad = jnp.stack(
        [
            jnp.sum(query_low.astype(jnp.float32), axis=0),
            jnp.sum(value_low.astype(jnp.float32), axis=0),
        ]
    )
    normed_grad = lax.dot_general(
        stacked_grad, qkv_weight, (((1,), (1,)), ((), ())), preferred_element_type=jnp.float32
    )
    back_three, gain_three, shift_three = norm_backward(
        normed_grad, normed_three, inverse_three, norm_gains[2], members
    )
    residual_grad = out_grad_full + back_three
    grad_two = residual_grad.astype(jnp.bfloat16).reshape(grid_shape)
    act_two_grad, weight_two_grad, bias_two_grad = conv_backward(
        grad_two, row_mask, conv_weights[1], taps_two
    )
    middle_grad, gain_two, shift_two = norm_backward(
        act_two_grad * swish_slope(pre_two), normed_two, inverse_two, norm_gains[1], members
    )
    grad_one = middle_grad.astype(jnp.bfloat16).reshape(grid_shape)
    act_one_grad, weight_one_grad, bias_one_grad = conv_backward(
        grad_one, row_mask, conv_weights[0], taps_one
    )
    input_back, gain_one, shift_one = norm_backward(
        act_one_grad * swish_slope(pre_one), normed_one, inverse_one, norm_gains[0], members
    )
    input_grad = residual_grad + input_back
    conv_grad = jnp.stack([weight_one_grad, weight_two_grad])
    conv_part = lax.psum_scatter(conv_grad, "height", scatter_dimension=4, tiled=True)
    conv_part = lax.psum_scatter(
        conv_part.astype(jnp.bfloat16), "canvas", scatter_dimension=3, tiled=True
    ).astype(jnp.float32)
    summed = lax.psum(
        (
            jnp.stack([gain_one, gain_two, gain_three]),
            jnp.stack([shift_one, shift_two, shift_three]),
            jnp.stack([bias_one_grad, bias_two_grad]),
            qkv_grad,
            qv_grad,
            proj_grad,
            proj_bias_grad,
        ),
        ("canvas", "height"),
    )
    return (
        output.astype(jnp.bfloat16).reshape((1,) + grid_shape),
        input_grad.astype(jnp.bfloat16).reshape((1,) + grid_shape),
        summed[0],
        summed[1],
        conv_part,
        summed[2],
        summed[3],
        summed[4],
        summed[5],
        summed[6],
    )


def fold(block):
    rows, width = block.shape
    return jnp.sum(block.reshape(rows // 8, 8, width), axis=0)


def group_lanes(block, group):
    lane = lax.broadcasted_iota(jnp.int32, block.shape, 1)
    width = block.shape[1]
    step = 1
    while step < group:
        above = pltpu.roll(block, step, 1)
        below = pltpu.roll(block, width - step, 1)
        block = block + jnp.where((lane & step) != 0, above, below)
        step *= 2
    return block


def group_mean(partial, members):
    spread = group_lanes(partial, partial.shape[1] // GROUPS)
    return jnp.sum(spread, axis=0, keepdims=True) * (1.0 / members)


def widen(block, width):
    return jnp.concatenate([block] * (width // block.shape[1]), axis=1)


def each_block(pixels, block, body, carry=0):
    def step(index, carry):
        return body(pl.ds(pl.multiple_of(index * block, block), block), carry)

    return lax.fori_loop(0, pixels // block, step, carry)


def each_chunk(pixels, body, carry):
    return each_block(pixels, CHUNK, body, carry)


def aligned(start, step):
    return start if isinstance(start, int) else pl.multiple_of(start, step)


def fold_about(block, center):
    rows, width = block.shape
    offset = block.reshape(rows // 8, 8, width) - center[None]
    return jnp.sum(offset, axis=0), jnp.sum(offset * offset, axis=0)


def finish_stats(center, sums, squares, pixels):
    width = center.shape[1] // GROUPS
    share = pixels / 8.0
    means = center + sums * (1.0 / share)
    spread = squares - sums * sums * (1.0 / share)
    mean = group_mean(means, 8.0 * width)
    offset = means - mean
    variance = group_mean(spread + share * offset * offset, float(pixels * width))
    return mean, lax.rsqrt(variance + epsilon)


class RunningStats:
    def __init__(self):
        self.center = None

    def add(self, block):
        if self.center is None:
            self.center = block[0:8]
            self.sums, self.squares = fold_about(block, self.center)
        else:
            sums, squares = fold_about(block, self.center)
            self.sums, self.squares = self.sums + sums, self.squares + squares

    def finish(self, pixels):
        return finish_stats(self.center, self.sums, self.squares, pixels)


def put_taps(taps_ref, block, rows, cols):
    count, channels = block.shape
    place = lax.broadcasted_iota(jnp.int32, block.shape, 0) & (cols - 1)
    left = jnp.where(place == 0, 0.0, pltpu.roll(block, 1, 0))
    right = jnp.where(place == cols - 1, 0.0, pltpu.roll(block, count - 1, 0))
    inner = pl.ds(aligned(rows.start + cols, cols), count)
    taps_ref[inner, 0:channels] = left.astype(jnp.bfloat16)
    taps_ref[inner, channels : 2 * channels] = block.astype(jnp.bfloat16)
    taps_ref[inner, 2 * channels :] = right.astype(jnp.bfloat16)


def clear_edges(taps_ref, cols):
    edge = jnp.zeros((cols, taps_ref.shape[1]), taps_ref.dtype)
    taps_ref[0:cols, :] = edge
    taps_ref[taps_ref.shape[0] - cols :, :] = edge


def run_conv(taps_ref, product, mask_ref, total_ref, fill, first, last, cols):
    pixels, channels = total_ref.shape
    for start in range(0, pixels, FILL_ROWS):
        for inner in range(start, start + FILL_ROWS, CHUNK):
            fill(pl.ds(inner, CHUNK))
        rows = pl.ds(start, FILL_ROWS)
        total_ref[rows, :] = first(rows, product(taps_ref, pl.ds(start + cols, FILL_ROWS), 1))
    block = min(CONV_ROWS, pixels)
    for row_tap in (0, 2):
        for start in range(0, pixels, block):
            rows = pl.ds(start, block)
            part = product(taps_ref, pl.ds(start + row_tap * cols, block), row_tap)
            mask = widen(mask_ref[row_tap // 2, rows, :], channels)
            value = total_ref[rows, :] + mask * part
            total_ref[rows, :] = value if row_tap == 0 else last(rows, value)


def product_forward(weight_ref):
    channels = weight_ref.shape[-1]

    def product(taps_ref, shifted, row_tap):
        return jnp.dot(
            taps_ref[shifted, :],
            weight_ref[row_tap].reshape(3 * channels, channels),
            preferred_element_type=jnp.float32,
        )

    return product


def product_backward(weight_ref):
    def product(taps_ref, shifted, row_tap):
        return lax.dot_general(
            taps_ref[shifted, :],
            weight_ref[row_tap],
            (((1,), (1,)), ((), ())),
            preferred_element_type=jnp.float32,
        )

    return product


def smooth(values):
    part = 0.5 * jnp.tanh(0.5 * values) + 0.5
    return values * part, part


def activation(read, mean, inverse, gain, shift, act_ref, taps_ref, cols):
    scale = inverse * gain

    def fill(rows):
        act = smooth((read(rows) - mean) * scale + shift)[0]
        act_ref[rows, :] = act.astype(jnp.bfloat16)
        put_taps(taps_ref, act, rows, cols)

    return fill


def back_means(sums, gain, pixels):
    channels = gain.shape[1]
    members = float(pixels * (channels // GROUPS))
    return group_mean(sums[0] * gain, members), group_mean(sums[1] * gain, members)


def column_total(partial):
    return jnp.sum(partial, axis=0, keepdims=True)


def weight_part(act_ref, grad_ref, lanes_ref, flip_ref, columns_ref, part_ref, cols):
    pixels, channels = act_ref.shape
    height = lax.axis_index("height")
    share = NARROW // 2
    block = pl.ds(pl.multiple_of((height // 2) * NARROW, NARROW), NARROW)
    flip_ref[...] = grad_ref[:, block].T
    own = pl.ds(pl.multiple_of((height % 2) * share, share), share)
    grad = flip_ref[own, :].astype(jnp.float32)
    place = lax.broadcasted_iota(jnp.int32, grad.shape, 1) & (cols - 1)
    for col_tap in range(3):
        shifted = grad
        if col_tap == 0:
            shifted = jnp.where(place == cols - 1, 0.0, pltpu.roll(grad, pixels - 1, 1))
        elif col_tap == 2:
            shifted = jnp.where(place == 0, 0.0, pltpu.roll(grad, 1, 1))
        for row_tap in range(3):
            moved = shifted
            if row_tap == 0:
                moved = pltpu.roll(shifted, pixels - cols, 1) * lanes_ref[1:2, :]
            elif row_tap == 2:
                moved = pltpu.roll(shifted, cols, 1) * lanes_ref[0:1, :]
            tap = 3 * row_tap + col_tap
            columns_ref[tap * share : (tap + 1) * share, :] = moved.astype(jnp.bfloat16)
    part_ref[...] = jnp.dot(
        columns_ref[...], act_ref[...], preferred_element_type=jnp.float32
    ).astype(jnp.bfloat16)


def conv_back(grad_ref, weights_ref, mask_ref, taps_ref, total_ref, read, table_ref, which, cols):
    clear_edges(taps_ref, cols)
    mean, inverse, gain, shift = norm_rows(table_ref, which)
    sums = []

    def fill(rows):
        put_taps(taps_ref, grad_ref[rows, :].astype(jnp.float32), rows, cols)

    def slope(rows, value):
        normed = (read(rows) - mean) * inverse
        pre = normed * gain + shift
        part = smooth(pre)[1]
        grad = value * (part * (1.0 + pre * (1.0 - part)))
        sums.append((fold(grad), fold(grad * normed)))
        return grad

    run_conv(
        taps_ref,
        product_backward(weights_ref),
        mask_ref,
        total_ref,
        fill,
        lambda rows, part: part,
        slope,
        cols,
    )
    return sum(pair[0] for pair in sums), sum(pair[1] for pair in sums)


def norm_back(total_ref, sums, read, table_ref, which):
    mean, inverse, gain, shift = norm_rows(table_ref, which)
    mean_grad, mean_cross = back_means(sums, gain, total_ref.shape[0])

    def back(rows):
        normed = (read(rows) - mean) * inverse
        return inverse * (total_ref[rows, :] * gain - mean_grad - normed * mean_cross)

    return back


def turn_kernel(
    grad_ref, mask_ref, weights_ref, middle_ref, table_ref, total_ref, sums_ref, taps_ref, *, cols
):
    sums_ref[0:8, :], sums_ref[8:16, :] = conv_back(
        grad_ref,
        weights_ref.at[1],
        mask_ref,
        taps_ref,
        total_ref,
        lambda rows: middle_ref[rows, :],
        table_ref,
        1,
        cols,
    )


def norm_rows(table_ref, which):
    picks = (2 * which, 2 * which + 1, 6 + which, 9 + which)
    return tuple(table_ref[pick : pick + 1, :] for pick in picks)


def build_masks(ids_ref, mask_ref, lanes_ref, id_rows_ref, id_cols_ref, cols):
    rows = ids_ref.shape[1]
    for row in range(rows):
        here = ids_ref[0, row]
        place = slice(row * cols, (row + 1) * cols)
        id_rows_ref[place, :] = jnp.full((cols, LANES), here, jnp.int32)
        for side, other in ((0, row - 1), (1, row + 1)):
            same = jnp.float32(0.0)
            if 0 <= other < rows:
                same = jnp.where(ids_ref[0, other] == here, 1.0, 0.0).astype(jnp.float32)
            mask_ref[side, place, :] = jnp.full((cols, LANES), same, jnp.float32)
    lane = lax.broadcasted_iota(jnp.int32, (8, LANES), 1)
    each = LANES // cols
    for block in range(rows // each):
        ids = jnp.full((8, LANES), ids_ref[0, block * each], jnp.int32)
        for step in range(1, each):
            ids = jnp.where(lane >= step * cols, ids_ref[0, block * each + step], ids)
        id_cols_ref[:, block * LANES : (block + 1) * LANES] = ids
    ids = id_cols_ref[...].astype(jnp.float32)
    pixels = ids.shape[1]
    pixel = lax.broadcasted_iota(jnp.int32, ids.shape, 1)
    above = jnp.where(pixel < cols, -1.0, pltpu.roll(ids, cols, 1))
    below = jnp.where(pixel >= pixels - cols, -1.0, pltpu.roll(ids, pixels - cols, 1))
    lanes_ref[0:1, :] = jnp.where(above == ids, 1.0, 0.0)[0:1]
    lanes_ref[1:2, :] = jnp.where(below == ids, 1.0, 0.0)[0:1]


def place_pieces(pieces, whole_ref, sems):
    own_pixels = whole_ref.shape[0] // len(pieces)
    height = lax.axis_index("height")
    copies = []
    for place, piece in enumerate(pieces):
        start = pl.multiple_of((height ^ place) * own_pixels, own_pixels)
        rows = pl.ds(start, own_pixels)
        copies.append(pltpu.make_async_copy(piece, whole_ref.at[rows, :], sems.at[place]))
    return copies


def hold_kernel(
    ids_hbm,
    gains_hbm,
    shifts_hbm,
    biases_hbm,
    weights_hbm,
    qkv_hbm,
    proj_hbm,
    qv_bias_hbm,
    proj_bias_hbm,
    weights_ref,
    turned_ref,
    qkv_ref,
    proj_ref,
    table_ref,
    mask_ref,
    lanes_ref,
    id_rows_ref,
    id_cols_ref,
    ids_ref,
    gains_ref,
    shifts_ref,
    biases_ref,
    qv_bias_ref,
    proj_bias_ref,
    sems,
    *,
    cols,
):
    channels = weights_ref.shape[-1]
    small = [
        (ids_hbm, ids_ref),
        (gains_hbm, gains_ref),
        (shifts_hbm, shifts_ref),
        (biases_hbm, biases_ref),
        (qv_bias_hbm, qv_bias_ref),
        (proj_bias_hbm, proj_bias_ref),
    ]
    large = [(weights_hbm, weights_ref), (qkv_hbm, qkv_ref), (proj_hbm, proj_ref)]
    for which in range(2):
        for row_tap in range(3):
            for col_tap in range(3):
                place = slice(col_tap * channels, (col_tap + 1) * channels)
                large.append(
                    (
                        weights_hbm.at[which, 2 - row_tap, 2 - col_tap],
                        turned_ref.at[which, row_tap, :, place],
                    )
                )
    copies = [
        pltpu.make_async_copy(source, target, sems.at[index])
        for index, (source, target) in enumerate(small + large)
    ]
    for copy in copies:
        copy.start()
    for copy in copies[: len(small)]:
        copy.wait()
    build_masks(ids_ref, mask_ref, lanes_ref, id_rows_ref, id_cols_ref, cols)
    table_ref[6:9, :] = gains_ref[...]
    table_ref[9:12, :] = shifts_ref[...]
    table_ref[12:14, :] = biases_ref[...]
    table_ref[14:16, :] = qv_bias_ref[...]
    table_ref[16:17, :] = proj_bias_ref[...]
    for copy in copies[len(small) :]:
        copy.wait()


def conv_kernel(*refs, cols, count):
    pieces, refs = refs[:count], refs[count:]
    (
        weights_ref,
        params_ref,
        mask_ref,
        features_ref,
        act_one_ref,
        middle_ref,
        act_two_ref,
        residual_ref,
        table_ref,
        own_ref,
        taps_ref,
        sem,
    ) = refs
    pixels, channels = features_ref.shape
    wide = jnp.float32
    own_copy = pltpu.make_async_copy(pieces[0], own_ref, sem)
    own_copy.start()
    table_ref[...] = params_ref[...]
    clear_edges(taps_ref, cols)

    def read_input(rows):
        return features_ref[rows, :].astype(wide)

    def read_middle(rows):
        return middle_ref[rows, :]

    height = lax.axis_index("height")
    own_pixels = pixels // count
    seen = RunningStats()
    for place in list(range(1, count)) + [0]:
        if place == 0:
            own_copy.wait()
        piece = (pieces[place] if place else own_ref)[...]
        start = pl.multiple_of((height ^ place) * own_pixels, own_pixels)
        features_ref[pl.ds(start, own_pixels), :] = piece
        seen.add(piece.astype(wide))
    table_ref[0:1, :], table_ref[1:2, :] = seen.finish(pixels)
    seen = RunningStats()

    def keep(rows, value):
        seen.add(value)
        return value

    run_conv(
        taps_ref,
        product_forward(weights_ref.at[0]),
        mask_ref,
        middle_ref,
        activation(read_input, *norm_rows(table_ref, 0), act_one_ref, taps_ref, cols),
        lambda rows, part: part + table_ref[12:13, :],
        keep,
        cols,
    )
    table_ref[2:3, :], table_ref[3:4, :] = seen.finish(pixels)
    seen = RunningStats()
    run_conv(
        taps_ref,
        product_forward(weights_ref.at[1]),
        mask_ref,
        residual_ref,
        activation(read_middle, *norm_rows(table_ref, 1), act_two_ref, taps_ref, cols),
        lambda rows, part: part + (read_input(rows) + table_ref[13:14, :]),
        keep,
        cols,
    )
    table_ref[4:5, :], table_ref[5:6, :] = seen.finish(pixels)


def score_kernel(
    qkv_ref,
    proj_ref,
    residual_ref,
    table_ref,
    id_rows_ref,
    id_cols_ref,
    normed_ref,
    query_ref,
    key_ref,
    value_ref,
    soft_ref,
    out_flip_ref,
    output_ref,
    value_flip_ref,
    scores_ref,
    *,
    score_scale,
):
    pixels, channels = residual_ref.shape
    own_pixels = output_ref.shape[0]
    wide = jnp.float32
    exponent = score_scale * 1.4426950408889634
    mean, inverse, gain, shift = norm_rows(table_ref, 2)
    scale = inverse * gain
    block = min(QUERY_ROWS, pixels)

    def project(rows, carry):
        normed = ((residual_ref[rows, :] - mean) * scale + shift).astype(jnp.bfloat16)
        normed_ref[rows, :] = normed
        query_ref[rows, :] = (
            jnp.dot(normed, qkv_ref[:, 0:channels], preferred_element_type=wide)
            + table_ref[14:15, :]
        ).astype(jnp.bfloat16)
        key_ref[rows, :] = jnp.dot(
            normed, qkv_ref[:, channels : 2 * channels], preferred_element_type=wide
        ).astype(jnp.bfloat16)
        values = (
            jnp.dot(normed, qkv_ref[:, 2 * channels :], preferred_element_type=wide)
            + table_ref[15:16, :]
        ).astype(jnp.bfloat16)
        value_ref[rows, :] = values
        value_flip_ref[:, rows] = values.T
        return carry

    each_block(pixels, block, project)

    def attend(rows, carry):
        def score(keys, peak):
            scores = lax.dot_general(
                key_ref[keys, :],
                query_ref[rows, :],
                (((1,), (1,)), ((), ())),
                preferred_element_type=wide,
            )
            same = widen(id_rows_ref[keys, :], block) == id_cols_ref[0:1, rows]
            scores = jnp.where(same, scores, masked_score)
            scores_ref[keys, :] = scores
            return jnp.maximum(peak, jnp.max(scores.reshape(-1, 8, block), axis=0))

        start = jnp.full((8, block), masked_score, wide)
        peak = jnp.max(each_block(pixels, KEY_ROWS, score, start), axis=0, keepdims=True)

        def raise_power(keys, total):
            powers = jnp.exp2((scores_ref[keys, :] - peak) * exponent)
            scores_ref[keys, :] = powers
            return total + fold(powers)

        zeros = jnp.zeros((8, block), wide)
        total = column_total(each_block(pixels, KEY_ROWS, raise_power, zeros))
        share = 1.0 / total

        def soften(keys, carry):
            soft_ref[keys, rows] = (scores_ref[keys, :] * share).astype(jnp.bfloat16)
            return carry

        each_block(pixels, KEY_ROWS, soften)
        out_flip_ref[:, rows] = jnp.dot(
            value_flip_ref[...], soft_ref[:, rows], preferred_element_type=wide
        ).astype(jnp.bfloat16)
        return carry

    each_block(pixels, block, attend)
    height = lax.axis_index("height")
    own = pl.ds(pl.multiple_of(height * own_pixels, own_pixels), own_pixels)
    output_ref[...] = (
        residual_ref[own, :]
        + lax.dot_general(
            out_flip_ref[:, own],
            proj_ref[...],
            (((0,), (0,)), ((), ())),
            preferred_element_type=wide,
        )
        + table_ref[16:17, :]
    ).astype(jnp.bfloat16)


def own_quarter():
    height = lax.axis_index("height")
    return (height & 1) * 2 + ((height >> 1) & 1)


def send_order(source_ref, targets, axis, share):
    me = lax.axis_index("canvas")
    for step, target in enumerate(targets):
        place = pl.ds(pl.multiple_of((me ^ step) * share, share), share)
        target[...] = source_ref[place, :] if axis == 0 else source_ref[:, place]


def attention_kernel(
    proj_ref,
    normed_ref,
    query_ref,
    key_ref,
    value_ref,
    soft_ref,
    out_flip_ref,
    *refs,
    score_scale,
    count,
):
    pieces, (grad_ref, packed_ref, sums_ref), refs = (
        refs[:count],
        refs[count : count + 3],
        refs[count + 3 :],
    )
    *mixed_refs, mixed_ref, key_flip_ref, back_ref, score_grad_ref, flip_ref, sems = refs
    pixels, channels = normed_ref.shape
    block = min(QUERY_ROWS, pixels)
    wide = jnp.float32
    copies = place_pieces(pieces, grad_ref, sems)
    for copy in copies:
        copy.start()
    quarter = channels // 4
    own = pl.ds(pl.multiple_of(own_quarter() * quarter, quarter), quarter)
    flip_ref[...] = normed_ref[:, own].T
    key_flip_ref[...] = key_ref[...].T
    for copy in copies:
        copy.wait()

    for start in range(0, pixels, block):
        rows = slice(start, start + block)
        back_ref[rows, :] = lax.dot_general(
            grad_ref[rows, :], proj_ref[...], (((1,), (1,)), ((), ())), preferred_element_type=wide
        ).astype(jnp.bfloat16)
    for start in range(0, pixels, block):
        rows = slice(start, start + block)
        weights = soft_ref[:, rows].astype(wide)
        weight_grad = lax.dot_general(
            value_ref[...],
            back_ref[rows, :],
            (((1,), (1,)), ((), ())),
            preferred_element_type=wide,
        )
        dots = jnp.sum(weights * weight_grad, axis=0, keepdims=True)
        score_grad = (weights * (weight_grad - dots)).astype(jnp.bfloat16)
        score_grad_ref[:, rows] = score_grad
        query_grad = jnp.dot(key_flip_ref[...], score_grad, preferred_element_type=wide)
        packed_ref[rows, 0:channels] = (query_grad * score_scale).astype(jnp.bfloat16).T
        packed_ref[rows, 2 * channels :] = jnp.dot(
            soft_ref[rows, :], back_ref[...], preferred_element_type=wide
        ).astype(jnp.bfloat16)
    for start in range(0, pixels, block):
        rows = slice(start, start + block)
        packed_ref[rows, channels : 2 * channels] = (
            jnp.dot(score_grad_ref[rows, :], query_ref[...], preferred_element_type=wide)
            * score_scale
        ).astype(jnp.bfloat16)

    def pack(rows, carry):
        return (
            carry[0] + fold(packed_ref[rows, 0:channels].astype(wide)),
            carry[1] + fold(packed_ref[rows, 2 * channels :].astype(wide)),
            carry[2] + fold(grad_ref[rows, :].astype(wide)),
        )

    zeros = jnp.zeros((8, channels), wide)
    totals = zeros, zeros, zeros
    for start in range(0, pixels, CHUNK):
        totals = pack(pl.ds(start, CHUNK), totals)
    sums_ref[...] = jnp.zeros(sums_ref.shape, wide)
    for row, total in enumerate(totals):
        sums_ref[8 + row : 9 + row, :] = column_total(total)
    mixed_ref[:, 0 : 3 * channels] = jnp.dot(
        flip_ref[...], packed_ref[...], preferred_element_type=wide
    ).astype(jnp.bfloat16)
    mixed_ref[:, 3 * channels :] = jnp.dot(
        out_flip_ref[own, :], grad_ref[...], preferred_element_type=wide
    ).astype(jnp.bfloat16)
    send_order(mixed_ref, mixed_refs, 0, quarter // len(mixed_refs))


def third_kernel(
    qkv_ref,
    grad_ref,
    packed_ref,
    residual_ref,
    table_ref,
    act_two_ref,
    lanes_ref,
    old_sums_ref,
    residual_grad_ref,
    grad_two_ref,
    sums_ref,
    part_ref,
    total_ref,
    flip_ref,
    columns_ref,
    *,
    cols,
):
    pixels, channels = residual_ref.shape
    block = pixels
    wide = jnp.float32
    mean, inverse, gain, shift = norm_rows(table_ref, 2)
    zeros = jnp.zeros((8, channels), wide)

    sums = (zeros, zeros)
    for start in range(0, pixels, block):
        rows = pl.ds(start, block)
        normed_grad = lax.dot_general(
            packed_ref[rows, :], qkv_ref[...], (((1,), (1,)), ((), ())), preferred_element_type=wide
        )
        total_ref[rows, :] = normed_grad
        normed = (residual_ref[rows, :] - mean) * inverse
        sums = sums[0] + fold(normed_grad), sums[1] + fold(normed_grad * normed)
    sums_ref[...] = old_sums_ref[...]
    sums_ref[5:6, :] = column_total(sums[1])
    sums_ref[6:7, :] = column_total(sums[0])
    mean_grad, mean_cross = back_means(sums, gain, pixels)

    def finish(rows, carry):
        normed = (residual_ref[rows, :] - mean) * inverse
        back = inverse * (total_ref[rows, :] * gain - mean_grad - normed * mean_cross)
        total = grad_ref[rows, :].astype(wide) + back
        residual_grad_ref[rows, :] = total
        low = total.astype(jnp.bfloat16)
        grad_two_ref[rows, :] = low
        return carry + fold(low.astype(wide))

    sums_ref[7:8, :] = column_total(each_chunk(pixels, finish, zeros))
    weight_part(act_two_ref, grad_two_ref, lanes_ref, flip_ref, columns_ref, part_ref, cols)


def second_kernel(
    total_ref,
    partial_ref,
    middle_ref,
    table_ref,
    act_one_ref,
    lanes_ref,
    old_sums_ref,
    part_two_ref,
    grad_one_ref,
    sums_ref,
    keep_one_ref,
    send_one_ref,
    keep_two_ref,
    send_two_ref,
    flip_ref,
    columns_ref,
    part_ref,
    *,
    cols,
):
    pixels, channels = middle_ref.shape
    sums = partial_ref[0:8, :], partial_ref[8:16, :]
    back = norm_back(total_ref, sums, lambda rows: middle_ref[rows, :], table_ref, 1)
    sums_ref[...] = old_sums_ref[...]
    sums_ref[2:3, :] = column_total(sums[1])
    sums_ref[3:4, :] = column_total(sums[0])

    def finish(rows, carry):
        low = back(rows).astype(jnp.bfloat16)
        grad_one_ref[rows, :] = low
        return carry + fold(low.astype(jnp.float32))

    zeros = jnp.zeros((8, channels), jnp.float32)
    sums_ref[4:5, :] = column_total(each_chunk(pixels, finish, zeros))
    weight_part(act_one_ref, grad_one_ref, lanes_ref, flip_ref, columns_ref, part_ref, cols)
    me = lax.axis_index("canvas")
    rows = part_ref.shape[0]
    for source_ref, near, far, keep_ref, send_ref in (
        (part_ref, 1, 2, keep_one_ref, send_one_ref),
        (part_two_ref, 2, 1, keep_two_ref, send_two_ref),
    ):
        width = keep_ref.shape[1]
        for target_ref, flip in ((keep_ref, 0), (send_ref, near)):
            for slot in range(2):
                owner = me ^ flip ^ (slot * far)
                place = pl.ds(pl.multiple_of(owner * width, width), width)
                target_ref[slot * rows : (slot + 1) * rows, :] = source_ref[:, place]


def first_kernel(
    grad_one_ref,
    features_ref,
    table_ref,
    mask_ref,
    old_sums_ref,
    weights_ref,
    own_ref,
    sums_ref,
    partial_ref,
    taps_ref,
    total_ref,
    *,
    cols,
):
    def read(rows):
        return features_ref[rows, :].astype(jnp.float32)

    sums = conv_back(
        grad_one_ref, weights_ref.at[0], mask_ref, taps_ref, total_ref, read, table_ref, 0, cols
    )
    partial_ref[0:8, :], partial_ref[8:16, :] = sums
    sums_ref[...] = old_sums_ref[...]
    sums_ref[0:1, :] = column_total(sums[1])
    sums_ref[1:2, :] = column_total(sums[0])
    count = own_ref.shape[0]
    own = pl.ds(pl.multiple_of(lax.axis_index("height") * count, count), count)
    own_ref[...] = total_ref[own, :]


def own_kernel(
    own_ref,
    partial_ref,
    features_ref,
    residual_grad_ref,
    table_ref,
    packed_ref,
    old_qkv,
    old_proj,
    input_grad_ref,
    qkv_hbm,
    proj_hbm,
    qkv_ref,
    proj_ref,
    sems,
):
    copies = spread_quarters([packed_ref], [2], qkv_ref, proj_ref, qkv_hbm, proj_hbm, sems)
    mean, inverse, gain, shift = norm_rows(table_ref, 0)
    pixels = features_ref.shape[0]
    sums = partial_ref[0:8, :], partial_ref[8:16, :]
    mean_grad, mean_cross = back_means(sums, gain, pixels)
    count = own_ref.shape[0]
    own = pl.ds(pl.multiple_of(lax.axis_index("height") * count, count), count)
    normed = (features_ref[own, :].astype(jnp.float32) - mean) * inverse
    back = inverse * (own_ref[...] * gain - mean_grad - normed * mean_cross)
    input_grad_ref[...] = (residual_grad_ref[own, :] + back).astype(jnp.bfloat16)
    for copy in copies:
        copy.wait()


def place_kernel(*refs):
    joints, (qkv_hbm, proj_hbm, packed_ref, qkv_ref, proj_ref, sems) = refs[:-6], refs[-6:]
    share = packed_ref.shape[0] // len(joints)
    me = lax.axis_index("canvas")
    for step, joint in enumerate(joints):
        place = pl.ds(pl.multiple_of((me ^ step) * share, share), share)
        packed_ref[place, :] = joint[...]
    copies = spread_quarters([packed_ref], [0], qkv_ref, proj_ref, qkv_hbm, proj_hbm, sems)
    for copy in copies:
        copy.wait()


def spread_quarters(packed, flips, qkv_ref, proj_ref, qkv_hbm, proj_hbm, sems):
    quarter = packed[0].shape[0]
    inner = qkv_ref.shape[2]
    copies = []
    for index, packed_ref in enumerate(packed):
        owner = own_quarter() ^ flips[index]
        rows = pl.ds(pl.multiple_of(owner * quarter, quarter), quarter)
        qkv_ref[index] = packed_ref[:, 0:inner].astype(jnp.float32)
        proj_ref[index] = packed_ref[:, inner:].astype(jnp.float32)
        for which, (held, target) in enumerate(((qkv_ref, qkv_hbm), (proj_ref, proj_hbm))):
            copy = pltpu.make_async_copy(held.at[index], target.at[rows, :], sems.at[index, which])
            copy.start()
            copies.append(copy)
    return copies


def join_kernel(
    old_qkv, old_proj, chip_ref, both_ref, qkv_hbm, proj_hbm, qkv_ref, proj_ref, sems
):
    copies = spread_quarters(
        [chip_ref, both_ref], [1, 3], qkv_ref, proj_ref, qkv_hbm, proj_hbm, sems
    )
    for copy in copies:
        copy.wait()


def halve_kernel(
    keep_one_ref,
    got_one_ref,
    keep_two_ref,
    got_two_ref,
    hold_one_ref,
    send_one_ref,
    hold_two_ref,
    send_two_ref,
):
    for keep_ref, got_ref, hold_ref, send_ref in (
        (keep_one_ref, got_one_ref, hold_one_ref, send_one_ref),
        (keep_two_ref, got_two_ref, hold_two_ref, send_two_ref),
    ):
        total = keep_ref[...].astype(jnp.float32) + got_ref[...].astype(jnp.float32)
        rows = hold_ref.shape[0]
        hold_ref[...] = total[0:rows]
        send_ref[...] = total[rows:].astype(jnp.bfloat16)


def sums_kernel(
    sums_ref,
    got_sums_ref,
    hold_one_ref,
    got_one_ref,
    hold_two_ref,
    got_two_ref,
    share_ref,
    gains_ref,
    shifts_ref,
    conv_ref,
    qv_ref,
    proj_ref,
):
    for which, (hold_ref, got_ref) in enumerate(
        ((hold_one_ref, got_one_ref), (hold_two_ref, got_two_ref))
    ):
        total = hold_ref[...] + got_ref[...].astype(jnp.float32)
        share_ref[which] = total.reshape(share_ref.shape[1:])
    total = sums_ref[...] + got_sums_ref[...]
    for row, start in enumerate((0, 2, 5)):
        gains_ref[row : row + 1, :] = total[start : start + 1]
        shifts_ref[row : row + 1, :] = total[start + 1 : start + 2]
    conv_ref[0:1, :] = total[4:5]
    conv_ref[1:2, :] = total[7:8]
    qv_ref[...] = total[8:10]
    proj_ref[...] = total[10:11]


def call_kernel(kernel, outputs, scratch, operands, places, flops, limit, out_places=None, aliases={}):
    out_places = out_places or "v" * len(outputs)
    spaces = {
        "v": pl.BlockSpec(memory_space=pltpu.VMEM),
        "s": pl.BlockSpec(memory_space=pltpu.SMEM),
        "h": pl.BlockSpec(memory_space=pl.ANY),
        "o": pl.BlockSpec(memory_space=pltpu.VMEM),
        "a": pl.BlockSpec(memory_space=pl.ANY),
    }
    moved = 8 * flops // LANES
    held = {"v": pltpu.VMEM, "h": pltpu.HBM, "o": jax.ShapeDtypeStruct}
    operands = [
        pltpu.with_memory_space_constraint(array, pltpu.HBM) if place == "h" else array
        for array, place in zip(operands, places)
    ]
    return pl.pallas_call(
        kernel,
        out_shape=[held[place](*output) for output, place in zip(outputs, out_places)],
        in_specs=[spaces[place] for place in places],
        out_specs=[spaces[place] for place in out_places],
        scratch_shapes=scratch,
        input_output_aliases=aliases,
        compiler_params=pltpu.CompilerParams(vmem_limit_bytes=limit * 2**20),
        cost_estimate=pl.CostEstimate(flops=flops, bytes_accessed=moved, transcendentals=0),
    )(*operands)


def send_height(block, step):
    size = lax.axis_size("height")
    return lax.ppermute(block, "height", [(i, i ^ step) for i in range(size)])


def with_cores(blocks):
    return [piece for block in blocks for piece in (block, send_height(block, 1))]


def send_canvas(block, step):
    size = lax.axis_size("canvas")
    return lax.ppermute(block, "canvas", [(i, i ^ step) for i in range(size)])


def trade_canvas(pieces):
    return [pieces[0]] + [send_canvas(piece, step) for step, piece in enumerate(pieces) if step]


def whole_canvas(
    features,
    tile_ids,
    norm_gains,
    norm_shifts,
    conv_weights,
    conv_biases,
    qkv_weight,
    qv_bias,
    proj_weight,
    proj_bias,
    cotangent,
):
    height_size = lax.axis_size("height")
    canvas_size = lax.axis_size("canvas")
    local_rows, cols, channels = features.shape[1:]
    all_rows = tile_ids.shape[1]
    pixels = all_rows * cols
    own_pixels = local_rows * cols
    out_share = channels // height_size
    ci_share = channels // canvas_size
    quarter = channels // 4
    row_share = quarter // canvas_size
    low, wide = jnp.bfloat16, jnp.float32

    own_features = features.reshape(own_pixels, channels)
    own_grad = cotangent.reshape(own_pixels, channels)
    steps = range(2, height_size, 2)
    held_features = [own_features] + [send_height(own_features, step) for step in steps]
    plane = ((pixels, channels), low)
    plane_wide = ((pixels, channels), wide)
    sums_shape = ((16, channels), wide)
    mixed_shapes = [((row_share, 4 * channels), low)] * canvas_size
    taps = pltpu.VMEM((pixels + 2 * cols, 3 * channels), low)
    held_wide = pltpu.VMEM((pixels, channels), wide)
    flipped = pltpu.VMEM((channels, pixels), low)
    narrow = pltpu.VMEM((NARROW, pixels), low)
    columns = pltpu.VMEM((9 * out_share, pixels), low)
    part_held = pltpu.VMEM((9 * out_share, channels), low)
    sem = pltpu.SemaphoreType.DMA
    conv_flops = 2 * 9 * pixels * channels * channels
    dot_flops = 2 * pixels * channels * channels
    score_flops = 2 * pixels * pixels * channels
    scale = channels ** (-0.5)

    (
        held_conv,
        turned,
        held_qkv,
        held_proj,
        params,
        mask,
        lane_mask,
        id_rows,
        id_cols,
    ) = call_kernel(
        functools.partial(hold_kernel, cols=cols),
        [
            (conv_weights.shape, low),
            ((2, 3, channels, 3 * channels), low),
            (qkv_weight.shape, low),
            (proj_weight.shape, low),
            ((24, channels), wide),
            ((2, pixels, LANES), wide),
            ((8, pixels), wide),
            ((pixels, LANES), jnp.int32),
            ((8, pixels), jnp.int32),
        ],
        [
            pltpu.SMEM(tile_ids.shape, jnp.int32),
            pltpu.VMEM(norm_gains.shape, wide),
            pltpu.VMEM(norm_shifts.shape, wide),
            pltpu.VMEM(conv_biases.shape, wide),
            pltpu.VMEM(qv_bias.shape, wide),
            pltpu.VMEM((1, channels), wide),
            sem((27,)),
        ],
        [
            tile_ids,
            norm_gains,
            norm_shifts,
            conv_biases,
            conv_weights,
            qkv_weight,
            proj_weight,
            qv_bias,
            proj_bias.reshape(1, channels),
        ],
        "h" * 9,
        conv_flops,
        8,
    )
    held_features[1:] = [
        lax.optimization_barrier((params, block))[1] for block in held_features[1:]
    ]
    pieces = with_cores(held_features)
    near_grad, pieces[2] = lax.optimization_barrier((own_grad, held_features[1]))
    far_grad, *pieces[4::2] = lax.optimization_barrier((own_grad, *held_features[2:]))
    held_grads = [own_grad, send_height(near_grad, 2)]
    held_grads += [send_height(far_grad, step) for step in steps[1:]]

    all_features, act_one, middle, act_two, residual, table = call_kernel(
        functools.partial(conv_kernel, cols=cols, count=height_size),
        [plane, plane, plane_wide, plane, plane_wide, ((24, channels), wide)],
        [pltpu.VMEM((own_pixels, channels), low), taps, sem],
        [*pieces, held_conv, params, mask],
        "h" + "v" * (height_size + 2),
        2 * conv_flops,
        16,
    )
    residual, *held_grads = lax.optimization_barrier((residual, *held_grads))
    grad_pieces = with_cores(held_grads)
    normed, query, key, value, soft, out_flip, output = call_kernel(
        functools.partial(score_kernel, score_scale=scale),
        [
            plane,
            plane,
            plane,
            plane,
            ((pixels, pixels), low),
            ((channels, pixels), low),
            ((own_pixels, channels), low),
        ],
        [
            flipped,
            pltpu.VMEM((pixels, min(QUERY_ROWS, pixels)), wide),
        ],
        [
            held_qkv,
            held_proj,
            residual,
            table,
            id_rows,
            id_cols,
        ],
        "vvvvvv",
        3 * dot_flops + 2 * score_flops,
        16,
        "v" * 6 + "o",
    )
    normed, *grad_pieces = lax.optimization_barrier((normed, *grad_pieces))
    all_grad, packed, sums, *mixed = call_kernel(
        functools.partial(attention_kernel, score_scale=scale, count=height_size),
        [plane, ((pixels, 3 * channels), low), sums_shape, *mixed_shapes],
        [
            pltpu.VMEM((quarter, 4 * channels), low),
            flipped,
            pltpu.VMEM((pixels, channels), low),
            pltpu.VMEM((pixels, pixels), low),
            pltpu.VMEM((quarter, pixels), low),
            sem((height_size,)),
        ],
        [held_proj, normed, query, key, value, soft, out_flip, *grad_pieces],
        "vvvvvvvh" + "a" * (height_size - 1),
        3 * dot_flops + 4 * score_flops,
        20,
    )
    mixed = trade_canvas(mixed)
    residual_grad, grad_two, sums, part_two = call_kernel(
        functools.partial(third_kernel, cols=cols),
        [plane_wide, plane, sums_shape, ((9 * out_share, channels), low)],
        [held_wide, narrow, columns],
        [held_qkv, all_grad, packed, residual, table, act_two, lane_mask, sums],
        "vvvvvvvv",
        3 * dot_flops + conv_flops // height_size,
        16,
    )
    grad_two, *mixed = lax.optimization_barrier((grad_two, *mixed))
    mixed_sum = mixed[0].astype(wide)
    for piece in mixed[1:]:
        mixed_sum = mixed_sum + piece.astype(wide)
    joints = trade_canvas([mixed_sum.astype(low)] * canvas_size)
    act_two_grad, partial_sums = call_kernel(
        functools.partial(turn_kernel, cols=cols),
        [plane_wide, sums_shape],
        [taps],
        [grad_two, mask, turned, middle, table],
        "vvvvv",
        conv_flops,
        16,
    )
    act_two_grad, *joints = lax.optimization_barrier((act_two_grad, *joints))
    qkv_grad, proj_grad, own_mixed = call_kernel(
        place_kernel,
        [(qkv_weight.shape, wide), (proj_weight.shape, wide), ((quarter, 4 * channels), low)],
        [
            pltpu.VMEM((1, quarter, 3 * channels), wide),
            pltpu.VMEM((1, quarter, channels), wide),
            sem((1, 2)),
        ],
        joints,
        "v" * canvas_size,
        0,
        12,
        "hhv",
    )
    chip_mixed = send_height(own_mixed, 2)
    core_mixed = send_height(own_mixed, 1)
    grad_one, sums, keep_one, send_one, keep_two, send_two = call_kernel(
        functools.partial(second_kernel, cols=cols),
        [plane, sums_shape] + [((18 * out_share, ci_share), low)] * 4,
        [narrow, columns, part_held],
        [act_two_grad, partial_sums, middle, table, act_one, lane_mask, sums, part_two],
        "vvvvvvvv",
        conv_flops // height_size,
        16,
    )
    got_one, got_two = send_canvas(send_one, 1), send_canvas(send_two, 2)
    own_total, sums, partial_sums = call_kernel(
        functools.partial(first_kernel, cols=cols),
        [((own_pixels, channels), wide), sums_shape, sums_shape],
        [taps, held_wide],
        [grad_one, all_features, table, mask, sums, turned],
        "vvvvvv",
        conv_flops,
        16,
    )
    sums, core_mixed, got_one, got_two = lax.optimization_barrier(
        (sums, core_mixed, got_one, got_two)
    )
    got_sums = send_canvas(sums, 1)
    hold_one, send_one, hold_two, send_two = call_kernel(
        halve_kernel,
        [((9 * out_share, ci_share), kind) for kind in (wide, low, wide, low)],
        [],
        [keep_one, got_one, keep_two, got_two],
        "vvvv",
        0,
        12,
    )
    got_one, got_two = send_canvas(send_one, 2), send_canvas(send_two, 1)
    own_total, hold_one = lax.optimization_barrier((own_total, hold_one))
    quarter_scratch = [
        pltpu.VMEM((2, quarter, 3 * channels), wide),
        pltpu.VMEM((2, quarter, channels), wide),
        sem((2, 2)),
    ]
    grad_shapes = [(qkv_weight.shape, wide), (proj_weight.shape, wide)]
    input_grad, qkv_grad, proj_grad = call_kernel(
        own_kernel,
        [((own_pixels, channels), low), *grad_shapes],
        quarter_scratch,
        [
            own_total,
            partial_sums,
            all_features,
            residual_grad,
            table,
            core_mixed,
            qkv_grad,
            proj_grad,
        ],
        "vvvvvvhh",
        dot_flops // 2,
        12,
        "ohh",
        {6: 1, 7: 2},
    )
    input_grad, got_sums, chip_mixed = lax.optimization_barrier((input_grad, got_sums, chip_mixed))
    both_mixed = send_height(chip_mixed, 1)
    sums = sums + got_sums
    got_sums = send_canvas(sums, 2)
    both_mixed, got_one, got_two = lax.optimization_barrier((both_mixed, got_one, got_two))
    qkv_grad, proj_grad = call_kernel(
        join_kernel,
        grad_shapes,
        quarter_scratch,
        [qkv_grad, proj_grad, chip_mixed, both_mixed],
        "hhvv",
        0,
        12,
        "hh",
        {0: 0, 1: 1},
    )
    qkv_grad, got_sums = lax.optimization_barrier((qkv_grad, got_sums))
    vector_shapes = [norm_gains.shape, norm_shifts.shape, conv_biases.shape, qv_bias.shape]
    conv_grad, gains_grad, shifts_grad, biases_grad, qv_grad, proj_bias_grad = call_kernel(
        sums_kernel,
        [((2, 3, 3, out_share, ci_share), wide)]
        + [(shape, wide) for shape in vector_shapes + [(1, channels)]],
        [],
        [sums, got_sums, hold_one, got_one, hold_two, got_two],
        "vvvvvv",
        0,
        12,
        "o" * 6,
    )
    own_shape = (1, local_rows, cols, channels)
    return (
        output.reshape(own_shape),
        input_grad.reshape(own_shape),
        gains_grad,
        shifts_grad,
        jnp.swapaxes(conv_grad, 3, 4),
        biases_grad,
        qkv_grad,
        qv_grad,
        proj_grad,
        proj_bias_grad.reshape(channels),
    )


def on_device(*arrays):
    features, tile_ids = arrays[0], arrays[1]
    local_rows, cols, channels = features.shape[1:]
    pixels = tile_ids.shape[1] * cols
    height_size, canvas_size = lax.axis_size("height"), lax.axis_size("canvas")
    powers = all(size & (size - 1) == 0 for size in (height_size, canvas_size, cols))
    fits = (
        powers
        and height_size > 2
        and canvas_size == 4
        and channels == LANES * canvas_size
        and pixels <= MOST_PIXELS
        and pixels % FILL_ROWS == 0
        and FILL_ROWS % CHUNK == 0
        and pixels % KEY_ROWS == 0
        and (local_rows * cols) % LANES == 0
        and CHUNK % cols == 0
        and cols % 16 == 0
        and channels % (LANES * canvas_size) == 0
        and 2 * channels == NARROW * height_size
    )
    return whole_canvas(*arrays) if fits else split_canvas(*arrays)


def solution(mesh):
    in_specs = (
        P("canvas", "height", None, None),
        P("canvas", None),
        P(),
        P(),
        P(),
        P(),
        P(),
        P(),
        P(),
        P(),
        P("canvas", "height", None, None),
    )
    out_specs = (
        P("canvas", "height", None, None),
        P("canvas", "height", None, None),
        P(),
        P(),
        P(None, None, None, "canvas", "height"),
        P(),
        P(),
        P(),
        P(),
        P(),
    )
    return jax.shard_map(
        on_device, mesh=mesh, in_specs=in_specs, out_specs=out_specs, check_vma=False
    )
```

```python
import functools

import jax
import jax.numpy as jnp
from jax import lax
from jax.experimental import pallas as pl
from jax.experimental.pallas import tpu as pltpu
from jax.sharding import PartitionSpec as P

GROUPS = 32


epsilon = 1e-06
masked_score = -1e30
MOST_PIXELS = 1024
LANES = 128
NARROW = 128
CHUNK = 128
CONV_ROWS = 1024
FILL_ROWS = 256
QUERY_ROWS = 512
KEY_ROWS = 256


def extended(block, sides, width):
    for axis, dim in sides:
        count = lax.axis_size(axis)
        forward = [(i, i + 1) for i in range(count - 1)]
        backward = [(target, source) for source, target in forward]
        low = lax.ppermute(
            lax.slice_in_dim(block, block.shape[dim] - width, None, axis=dim), axis, forward
        )
        high = lax.ppermute(lax.slice_in_dim(block, 0, width, axis=dim), axis, backward)
        block = jnp.concatenate([low, block, high], axis=dim)
    return block


def group_total(vector):
    return vector.reshape(GROUPS, -1).sum(axis=1)


def spread_groups(vector, channels):
    return jnp.repeat(vector, channels // GROUPS)


def norm_forward(values, gain, shift, members):
    channels = values.shape[1]
    totals = lax.psum(group_total(jnp.sum(values, axis=0)), "height")
    centered = values - spread_groups(totals / members, channels)
    squares = lax.psum(group_total(jnp.sum(centered * centered, axis=0)), "height")
    inverse = spread_groups(lax.rsqrt(squares / members + epsilon), channels)
    normed = centered * inverse
    return (normed, inverse, normed * gain + shift)


def norm_backward(grad_in, normed, inverse, gain, members):
    channels = grad_in.shape[1]
    scaled = grad_in * gain
    both_sums = lax.psum(
        (group_total(jnp.sum(scaled, axis=0)), group_total(jnp.sum(scaled * normed, axis=0))),
        "height",
    )
    mean_grad = spread_groups(both_sums[0] / members, channels)
    mean_cross = spread_groups(both_sums[1] / members, channels)
    result = inverse * (scaled - mean_grad - normed * mean_cross)
    return (result, jnp.sum(grad_in * normed, axis=0), jnp.sum(grad_in, axis=0))


def swish(values):
    return values * jax.nn.sigmoid(values)


def swish_slope(values):
    sigmoid_part = jax.nn.sigmoid(values)
    return sigmoid_part * (1.0 + values * (1.0 - sigmoid_part))


def tap_columns(padded, row_mask, local_rows, canvas_cols):
    pieces = []
    for row_tap in range(3):
        rows_taken = padded[row_tap : row_tap + local_rows] * row_mask[:, row_tap, None, None]
        for col_tap in range(3):
            pieces.append(rows_taken[:, col_tap : col_tap + canvas_cols])
    stacked = jnp.concatenate(pieces, axis=2)
    return stacked.reshape(local_rows * canvas_cols, stacked.shape[2])


def conv_forward(acts, row_mask, weight, bias):
    local_rows, canvas_cols, channels = acts.shape
    rimmed = extended(acts, (("height", 0),), 1)
    padded = jnp.pad(rimmed, ((0, 0), (1, 1), (0, 0)))
    gathered = tap_columns(padded, row_mask, local_rows, canvas_cols)
    result = (
        jnp.dot(
            gathered, weight.reshape(9 * channels, channels), preferred_element_type=jnp.float32
        )
        + bias
    )
    return (result, gathered)


def conv_backward(grad_low, row_mask, weight, gathered):
    local_rows, canvas_cols, channels = grad_low.shape
    flat_grad = grad_low.reshape(local_rows * canvas_cols, channels)
    weight_grad = lax.dot_general(
        gathered, flat_grad, (((0,), (0,)), ((), ())), preferred_element_type=jnp.float32
    )
    rimmed = extended(grad_low, (("height", 0),), 1)
    padded = jnp.pad(rimmed, ((0, 0), (1, 1), (0, 0)))
    grad_taps = tap_columns(padded, row_mask, local_rows, canvas_cols)
    flipped = jnp.transpose(weight[::-1, ::-1], (0, 1, 3, 2)).reshape(9 * channels, channels)
    input_part = jnp.dot(grad_taps, flipped, preferred_element_type=jnp.float32)
    return (
        input_part,
        weight_grad.reshape(3, 3, channels, channels),
        jnp.sum(flat_grad.astype(jnp.float32), axis=0),
    )


def take_rows(array, offset, count):
    return lax.dynamic_slice_in_dim(array, offset, count)


def score_grads(
    queries, out_grad, log_total, row_dots, query_ids, key_rows, value_rows, key_ids, score_scale
):
    scores = (
        lax.dot_general(
            queries, key_rows, (((1,), (1,)), ((), ())), preferred_element_type=jnp.float32
        )
        * score_scale
    )
    same_tile = query_ids[:, None] == key_ids[None, :]
    softmax_block = jnp.exp(jnp.where(same_tile, scores - log_total[:, None], masked_score))
    weight_grad = lax.dot_general(
        out_grad, value_rows, (((1,), (1,)), ((), ())), preferred_element_type=jnp.float32
    )
    score_grad = (softmax_block * (weight_grad - row_dots[:, None])).astype(jnp.bfloat16)
    return (softmax_block.astype(jnp.bfloat16), score_grad)


def split_canvas(
    features,
    tile_ids,
    norm_gains,
    norm_shifts,
    conv_weights,
    conv_biases,
    qkv_weight,
    qv_bias,
    proj_weight,
    proj_bias,
    cotangent,
):
    height_size = lax.axis_size("height")
    local_rows = features.shape[1]
    canvas_cols = features.shape[2]
    channels = features.shape[3]
    pixels = local_rows * canvas_cols
    row_ids = tile_ids[0]
    all_rows = row_ids.shape[0]
    members = float(all_rows * canvas_cols * (channels // GROUPS))
    score_scale = channels ** (-0.5)
    first_row = lax.axis_index("height") * local_rows
    edge_ids = jnp.full((1,), -1, jnp.int32)
    padded_ids = jnp.concatenate([edge_ids, row_ids, edge_ids])
    near_ids = lax.dynamic_slice_in_dim(padded_ids, first_row, local_rows + 2)
    own_rows = near_ids[1 : local_rows + 1]
    row_mask = jnp.stack(
        [near_ids[row_tap : row_tap + local_rows] == own_rows for row_tap in range(3)], axis=1
    ).astype(jnp.bfloat16)
    key_ids = jnp.repeat(row_ids, canvas_cols)
    query_ids = jnp.repeat(own_rows, canvas_cols)
    grid_shape = (local_rows, canvas_cols, channels)
    inputs = features[0].reshape(pixels, channels).astype(jnp.float32)
    normed_one, inverse_one, pre_one = norm_forward(inputs, norm_gains[0], norm_shifts[0], members)
    act_one = swish(pre_one).astype(jnp.bfloat16).reshape(grid_shape)
    middle, taps_one = conv_forward(act_one, row_mask, conv_weights[0], conv_biases[0])
    normed_two, inverse_two, pre_two = norm_forward(middle, norm_gains[1], norm_shifts[1], members)
    act_two = swish(pre_two).astype(jnp.bfloat16).reshape(grid_shape)
    branch, taps_two = conv_forward(act_two, row_mask, conv_weights[1], conv_biases[1])
    residual = inputs + branch
    normed_three, inverse_three, pre_three = norm_forward(
        residual, norm_gains[2], norm_shifts[2], members
    )
    attn_input = pre_three.astype(jnp.bfloat16)
    mixed = jnp.dot(attn_input, qkv_weight, preferred_element_type=jnp.float32)
    queries = (mixed[:, :channels] + qv_bias[0]).astype(jnp.bfloat16)
    key_rows = mixed[:, channels : 2 * channels].astype(jnp.bfloat16)
    value_rows = (mixed[:, 2 * channels :] + qv_bias[1]).astype(jnp.bfloat16)
    running_max = jnp.full((pixels,), masked_score, jnp.float32)
    key_piece = lax.all_gather(key_rows, "height", axis=0, tiled=True)
    value_piece = lax.all_gather(value_rows, "height", axis=0, tiled=True)
    scores = (
        lax.dot_general(
            queries, key_piece, (((1,), (1,)), ((), ())), preferred_element_type=jnp.float32
        )
        * score_scale
    )
    same_tile = query_ids[:, None] == key_ids[None, :]
    scores = jnp.where(same_tile, scores, masked_score)
    new_max = jnp.maximum(running_max, jnp.max(scores, axis=1))
    weights = jnp.where(same_tile, jnp.exp(scores - new_max[:, None]), 0.0)
    summed_out = jnp.dot(
        weights.astype(jnp.bfloat16), value_piece, preferred_element_type=jnp.float32
    )
    total_weight = jnp.sum(weights, axis=1)
    log_total = new_max + jnp.log(total_weight)
    attended = summed_out / total_weight[:, None]
    attended_low = attended.astype(jnp.bfloat16)
    output = (
        residual
        + jnp.dot(attended_low, proj_weight, preferred_element_type=jnp.float32)
        + proj_bias
    )
    out_grad = cotangent[0].reshape(pixels, channels)
    out_grad_full = out_grad.astype(jnp.float32)
    proj_grad = lax.dot_general(
        attended_low, out_grad, (((0,), (0,)), ((), ())), preferred_element_type=jnp.float32
    )
    proj_bias_grad = jnp.sum(out_grad_full, axis=0)
    attended_grad = lax.dot_general(
        out_grad, proj_weight, (((1,), (1,)), ((), ())), preferred_element_type=jnp.float32
    ).astype(jnp.bfloat16)
    row_dots = jnp.sum(attended_grad.astype(jnp.float32) * attended, axis=1)
    block_rows = pixels * min(height_size, 8)
    zero_block = jnp.zeros((pixels, channels), jnp.float32)
    key_all, value_all = (
        lax.all_gather(key_rows, "height", axis=0, tiled=True),
        lax.all_gather(value_rows, "height", axis=0, tiled=True),
    )
    query_all, grad_all = (
        lax.all_gather(queries, "height", axis=0, tiled=True),
        lax.all_gather(attended_grad, "height", axis=0, tiled=True),
    )
    total_all, dots_all = (
        lax.all_gather(log_total, "height", axis=0, tiled=True),
        lax.all_gather(row_dots, "height", axis=0, tiled=True),
    )

    def own_query_step(running, block_index):
        offset = block_index * block_rows
        key_part = take_rows(key_all, offset, block_rows)
        rounded, score_grad = score_grads(
            queries,
            attended_grad,
            log_total,
            row_dots,
            query_ids,
            key_part,
            take_rows(value_all, offset, block_rows),
            take_rows(key_ids, offset, block_rows),
            score_scale,
        )
        return (
            running
            + jnp.dot(score_grad, key_part, preferred_element_type=jnp.float32) * score_scale,
            None,
        )

    def own_key_step(running, block_index):
        offset = block_index * block_rows
        query_part = take_rows(query_all, offset, block_rows)
        grad_part = take_rows(grad_all, offset, block_rows)
        rounded, score_grad = score_grads(
            query_part,
            grad_part,
            take_rows(total_all, offset, block_rows),
            take_rows(dots_all, offset, block_rows),
            take_rows(key_ids, offset, block_rows),
            key_rows,
            value_rows,
            query_ids,
            score_scale,
        )
        key_part = (
            lax.dot_general(
                score_grad, query_part, (((0,), (0,)), ((), ())), preferred_element_type=jnp.float32
            )
            * score_scale
        )
        value_part = lax.dot_general(
            rounded, grad_part, (((0,), (0,)), ((), ())), preferred_element_type=jnp.float32
        )
        return ((running[0] + key_part, running[1] + value_part), None)

    block_count = key_all.shape[0] // block_rows
    query_grad, unused_one = lax.scan(own_query_step, zero_block, jnp.arange(block_count))
    (key_grad, value_grad), unused_two = lax.scan(
        own_key_step, (zero_block, zero_block), jnp.arange(block_count)
    )
    query_low = query_grad.astype(jnp.bfloat16)
    key_low = key_grad.astype(jnp.bfloat16)
    value_low = value_grad.astype(jnp.bfloat16)
    stacked_grad = jnp.concatenate([query_low, key_low, value_low], axis=1)
    qkv_grad = lax.dot_general(
        attn_input, stacked_grad, (((0,), (0,)), ((), ())), preferred_element_type=jnp.float32
    )
    qv_grad = jnp.stack(
        [
            jnp.sum(query_low.astype(jnp.float32), axis=0),
            jnp.sum(value_low.astype(jnp.float32), axis=0),
        ]
    )
    normed_grad = lax.dot_general(
        stacked_grad, qkv_weight, (((1,), (1,)), ((), ())), preferred_element_type=jnp.float32
    )
    back_three, gain_three, shift_three = norm_backward(
        normed_grad, normed_three, inverse_three, norm_gains[2], members
    )
    residual_grad = out_grad_full + back_three
    grad_two = residual_grad.astype(jnp.bfloat16).reshape(grid_shape)
    act_two_grad, weight_two_grad, bias_two_grad = conv_backward(
        grad_two, row_mask, conv_weights[1], taps_two
    )
    middle_grad, gain_two, shift_two = norm_backward(
        act_two_grad * swish_slope(pre_two), normed_two, inverse_two, norm_gains[1], members
    )
    grad_one = middle_grad.astype(jnp.bfloat16).reshape(grid_shape)
    act_one_grad, weight_one_grad, bias_one_grad = conv_backward(
        grad_one, row_mask, conv_weights[0], taps_one
    )
    input_back, gain_one, shift_one = norm_backward(
        act_one_grad * swish_slope(pre_one), normed_one, inverse_one, norm_gains[0], members
    )
    input_grad = residual_grad + input_back
    conv_grad = jnp.stack([weight_one_grad, weight_two_grad])
    conv_part = lax.psum_scatter(conv_grad, "height", scatter_dimension=4, tiled=True)
    conv_part = lax.psum_scatter(
        conv_part.astype(jnp.bfloat16), "canvas", scatter_dimension=3, tiled=True
    ).astype(jnp.float32)
    summed = lax.psum(
        (
            jnp.stack([gain_one, gain_two, gain_three]),
            jnp.stack([shift_one, shift_two, shift_three]),
            jnp.stack([bias_one_grad, bias_two_grad]),
            qkv_grad,
            qv_grad,
            proj_grad,
            proj_bias_grad,
        ),
        ("canvas", "height"),
    )
    return (
        output.astype(jnp.bfloat16).reshape((1,) + grid_shape),
        input_grad.astype(jnp.bfloat16).reshape((1,) + grid_shape),
        summed[0],
        summed[1],
        conv_part,
        summed[2],
        summed[3],
        summed[4],
        summed[5],
        summed[6],
    )


def fold(block):
    rows, width = block.shape
    return jnp.sum(block.reshape(rows // 8, 8, width), axis=0)


def group_lanes(block, group):
    lane = lax.broadcasted_iota(jnp.int32, block.shape, 1)
    width = block.shape[1]
    step = 1
    while step < group:
        above = pltpu.roll(block, step, 1)
        below = pltpu.roll(block, width - step, 1)
        block = block + jnp.where((lane & step) != 0, above, below)
        step *= 2
    return block


def group_mean(partial, members):
    spread = group_lanes(partial, partial.shape[1] // GROUPS)
    return jnp.sum(spread, axis=0, keepdims=True) * (1.0 / members)


def widen(block, width):
    return jnp.concatenate([block] * (width // block.shape[1]), axis=1)


def each_block(pixels, block, body, carry=0):
    def step(index, carry):
        return body(pl.ds(pl.multiple_of(index * block, block), block), carry)

    return lax.fori_loop(0, pixels // block, step, carry)


def each_chunk(pixels, body, carry):
    return each_block(pixels, CHUNK, body, carry)


def aligned(start, step):
    return start if isinstance(start, int) else pl.multiple_of(start, step)


def fold_about(block, center):
    rows, width = block.shape
    offset = block.reshape(rows // 8, 8, width) - center[None]
    return jnp.sum(offset, axis=0), jnp.sum(offset * offset, axis=0)


def finish_stats(center, sums, squares, pixels):
    width = center.shape[1] // GROUPS
    share = pixels / 8.0
    means = center + sums * (1.0 / share)
    spread = squares - sums * sums * (1.0 / share)
    mean = group_mean(means, 8.0 * width)
    offset = means - mean
    variance = group_mean(spread + share * offset * offset, float(pixels * width))
    return mean, lax.rsqrt(variance + epsilon)


class RunningStats:
    def __init__(self):
        self.center = None

    def add(self, block):
        if self.center is None:
            self.center = block[0:8]
            self.sums, self.squares = fold_about(block, self.center)
        else:
            sums, squares = fold_about(block, self.center)
            self.sums, self.squares = self.sums + sums, self.squares + squares

    def finish(self, pixels):
        return finish_stats(self.center, self.sums, self.squares, pixels)


def put_taps(taps_ref, block, rows, cols):
    count, channels = block.shape
    place = lax.broadcasted_iota(jnp.int32, block.shape, 0) & (cols - 1)
    left = jnp.where(place == 0, 0.0, pltpu.roll(block, 1, 0))
    right = jnp.where(place == cols - 1, 0.0, pltpu.roll(block, count - 1, 0))
    inner = pl.ds(aligned(rows.start + cols, cols), count)
    taps_ref[inner, 0:channels] = left.astype(jnp.bfloat16)
    taps_ref[inner, channels : 2 * channels] = block.astype(jnp.bfloat16)
    taps_ref[inner, 2 * channels :] = right.astype(jnp.bfloat16)


def clear_edges(taps_ref, cols):
    edge = jnp.zeros((cols, taps_ref.shape[1]), taps_ref.dtype)
    taps_ref[0:cols, :] = edge
    taps_ref[taps_ref.shape[0] - cols :, :] = edge


def begin_conv(taps_ref, product, total_ref, fill, first, cols):
    for start in range(0, total_ref.shape[0], FILL_ROWS):
        for inner in range(start, start + FILL_ROWS, CHUNK):
            fill(pl.ds(inner, CHUNK))
        rows = pl.ds(start, FILL_ROWS)
        total_ref[rows, :] = first(rows, product(taps_ref, pl.ds(start + cols, FILL_ROWS), 1))


def add_rows(taps_ref, product, mask_ref, total_ref, row_tap, last, cols, old_ref=None):
    pixels, channels = total_ref.shape
    rows = pl.ds(0, pixels)
    part = product(taps_ref, pl.ds(row_tap * cols, pixels), row_tap)
    old_ref = total_ref if old_ref is None else old_ref
    value = old_ref[...] + widen(mask_ref[row_tap // 2], channels) * part
    total_ref[...] = last(rows, value)


def run_conv(taps_ref, product, mask_ref, total_ref, fill, first, last, cols):
    begin_conv(taps_ref, product, total_ref, fill, first, cols)
    add_rows(taps_ref, product, mask_ref, total_ref, 0, lambda rows, value: value, cols)
    add_rows(taps_ref, product, mask_ref, total_ref, 2, last, cols)


def product_forward(weight_ref):
    channels = weight_ref.shape[-1]

    def product(taps_ref, shifted, row_tap):
        return jnp.dot(
            taps_ref[shifted, :],
            weight_ref[row_tap].reshape(3 * channels, channels),
            preferred_element_type=jnp.float32,
        )

    return product


def product_backward(weight_ref):
    def product(taps_ref, shifted, row_tap):
        return lax.dot_general(
            taps_ref[shifted, :],
            weight_ref[row_tap],
            (((1,), (1,)), ((), ())),
            preferred_element_type=jnp.float32,
        )

    return product


def smooth(values):
    part = 0.5 * jnp.tanh(0.5 * values) + 0.5
    return values * part, part


def activation(read, mean, inverse, gain, shift, act_ref, taps_ref, cols):
    scale = inverse * gain

    def fill(rows):
        act = smooth((read(rows) - mean) * scale + shift)[0]
        act_ref[rows, :] = act.astype(jnp.bfloat16)
        put_taps(taps_ref, act, rows, cols)

    return fill


def back_means(sums, gain, pixels):
    channels = gain.shape[1]
    members = float(pixels * (channels // GROUPS))
    return group_mean(sums[0] * gain, members), group_mean(sums[1] * gain, members)


def column_total(partial):
    return jnp.sum(partial, axis=0, keepdims=True)


def weight_part(act_ref, grad_ref, lanes_ref, flip_ref, columns_ref, part_ref, cols):
    pixels, channels = act_ref.shape
    height = lax.axis_index("height")
    share = NARROW // 2
    block = pl.ds(pl.multiple_of((height // 2) * NARROW, NARROW), NARROW)
    flip_ref[...] = grad_ref[:, block].T
    own = pl.ds(pl.multiple_of((height % 2) * share, share), share)
    grad = flip_ref[own, :].astype(jnp.float32)
    column = lax.broadcasted_iota(jnp.int32, grad.shape, 1) & (cols - 1)
    for col_tap in range(3):
        shifted = grad
        if col_tap == 0:
            shifted = jnp.where(column == cols - 1, 0.0, pltpu.roll(grad, pixels - 1, 1))
        elif col_tap == 2:
            shifted = jnp.where(column == 0, 0.0, pltpu.roll(grad, 1, 1))
        for row_tap in range(3):
            tap = 3 * row_tap + col_tap
            place = slice(tap * share, (tap + 1) * share)
            if row_tap == 1:
                columns_ref[place, :] = shifted.astype(jnp.bfloat16)
                continue
            side, turn = (0, pixels - cols) if row_tap == 0 else (1, cols)
            masked = (shifted * lanes_ref[side : side + 1, :]).astype(jnp.bfloat16)
            columns_ref[place, :] = pltpu.roll(masked, turn, 1)
    part_ref[...] = jnp.dot(
        columns_ref[...], act_ref[...], preferred_element_type=jnp.float32
    ).astype(jnp.bfloat16)


def begin_back(grad_ref, weights_ref, mask_ref, taps_ref, total_ref, cols):
    clear_edges(taps_ref, cols)

    def fill(rows):
        put_taps(taps_ref, grad_ref[rows, :].astype(jnp.float32), rows, cols)

    product = product_backward(weights_ref)
    begin_conv(taps_ref, product, total_ref, fill, lambda rows, part: part, cols)
    add_rows(taps_ref, product, mask_ref, total_ref, 0, lambda rows, value: value, cols)


def finish_back(
    weights_ref, mask_ref, taps_ref, total_ref, read, table_ref, which, cols, old_ref=None
):
    mean, inverse, gain, shift = norm_rows(table_ref, which)
    sums = []

    def slope(rows, value):
        normed = (read(rows) - mean) * inverse
        pre = normed * gain + shift
        part = smooth(pre)[1]
        grad = value * (part * (1.0 + pre * (1.0 - part)))
        sums.append((fold(grad), fold(grad * normed)))
        return grad

    add_rows(
        taps_ref, product_backward(weights_ref), mask_ref, total_ref, 2, slope, cols, old_ref
    )
    return sums[0]


def norm_back(total_ref, sums, read, table_ref, which):
    mean, inverse, gain, shift = norm_rows(table_ref, which)
    mean_grad, mean_cross = back_means(sums, gain, total_ref.shape[0])

    def back(rows):
        normed = (read(rows) - mean) * inverse
        return inverse * (total_ref[rows, :] * gain - mean_grad - normed * mean_cross)

    return back


def turn_kernel(
    grad_ref, mask_ref, weights_ref, middle_ref, table_ref, total_ref, sums_ref, taps_ref, *, cols
):
    begin_back(grad_ref, weights_ref.at[1], mask_ref, taps_ref, total_ref, cols)
    sums_ref[0:8, :], sums_ref[8:16, :] = finish_back(
        weights_ref.at[1],
        mask_ref,
        taps_ref,
        total_ref,
        lambda rows: middle_ref[rows, :],
        table_ref,
        1,
        cols,
    )


def norm_rows(table_ref, which):
    picks = (2 * which, 2 * which + 1, 6 + which, 9 + which)
    return tuple(table_ref[pick : pick + 1, :] for pick in picks)


def build_masks(ids_ref, mask_ref, lanes_ref, id_rows_ref, id_cols_ref, cols):
    rows = ids_ref.shape[1]
    for row in range(rows):
        here = ids_ref[0, row]
        place = slice(row * cols, (row + 1) * cols)
        id_rows_ref[place, :] = jnp.full((cols, LANES), here, jnp.int32)
        for side, other in ((0, row - 1), (1, row + 1)):
            same = jnp.float32(0.0)
            if 0 <= other < rows:
                same = jnp.where(ids_ref[0, other] == here, 1.0, 0.0).astype(jnp.float32)
            mask_ref[side, place, :] = jnp.full((cols, LANES), same, jnp.float32)
    lane = lax.broadcasted_iota(jnp.int32, (8, LANES), 1)
    each = LANES // cols
    for block in range(rows // each):
        ids = jnp.full((8, LANES), ids_ref[0, block * each], jnp.int32)
        for step in range(1, each):
            ids = jnp.where(lane >= step * cols, ids_ref[0, block * each + step], ids)
        id_cols_ref[:, block * LANES : (block + 1) * LANES] = ids
    ids = id_cols_ref[...].astype(jnp.float32)
    pixels = ids.shape[1]
    pixel = lax.broadcasted_iota(jnp.int32, ids.shape, 1)
    above = jnp.where(pixel < cols, -1.0, pltpu.roll(ids, cols, 1))
    below = jnp.where(pixel >= pixels - cols, -1.0, pltpu.roll(ids, pixels - cols, 1))
    lanes_ref[0:1, :] = jnp.where(above == ids, 1.0, 0.0)[0:1]
    lanes_ref[1:2, :] = jnp.where(below == ids, 1.0, 0.0)[0:1]


def place_pieces(pieces, whole_ref, sems):
    own_pixels = whole_ref.shape[0] // len(pieces)
    height = lax.axis_index("height")
    copies = []
    for place, piece in enumerate(pieces):
        start = pl.multiple_of((height ^ place) * own_pixels, own_pixels)
        rows = pl.ds(start, own_pixels)
        copies.append(pltpu.make_async_copy(piece, whole_ref.at[rows, :], sems.at[place]))
    return copies


def hold_kernel(
    ids_hbm,
    gains_hbm,
    shifts_hbm,
    biases_hbm,
    weights_hbm,
    qkv_hbm,
    proj_hbm,
    qv_bias_hbm,
    proj_bias_hbm,
    weights_ref,
    turned_ref,
    qkv_ref,
    proj_ref,
    table_ref,
    mask_ref,
    lanes_ref,
    id_rows_ref,
    id_cols_ref,
    ids_ref,
    gains_ref,
    shifts_ref,
    biases_ref,
    qv_bias_ref,
    proj_bias_ref,
    sems,
    *,
    cols,
):
    channels = weights_ref.shape[-1]
    small = [
        (ids_hbm, ids_ref),
        (gains_hbm, gains_ref),
        (shifts_hbm, shifts_ref),
        (biases_hbm, biases_ref),
        (qv_bias_hbm, qv_bias_ref),
        (proj_bias_hbm, proj_bias_ref),
    ]
    large = [(weights_hbm, weights_ref), (qkv_hbm, qkv_ref), (proj_hbm, proj_ref)]
    for which in range(2):
        for row_tap in range(3):
            for col_tap in range(3):
                place = slice(col_tap * channels, (col_tap + 1) * channels)
                large.append(
                    (
                        weights_hbm.at[which, 2 - row_tap, 2 - col_tap],
                        turned_ref.at[which, row_tap, :, place],
                    )
                )
    copies = [
        pltpu.make_async_copy(source, target, sems.at[index])
        for index, (source, target) in enumerate(small + large)
    ]
    for copy in copies:
        copy.start()
    for copy in copies[: len(small)]:
        copy.wait()
    build_masks(ids_ref, mask_ref, lanes_ref, id_rows_ref, id_cols_ref, cols)
    table_ref[6:9, :] = gains_ref[...]
    table_ref[9:12, :] = shifts_ref[...]
    table_ref[12:14, :] = biases_ref[...]
    table_ref[14:16, :] = qv_bias_ref[...]
    table_ref[16:17, :] = proj_bias_ref[...]
    for copy in copies[len(small) :]:
        copy.wait()


def conv_kernel(*refs, cols, count):
    pieces, refs = refs[:count], refs[count:]
    (
        weights_ref,
        params_ref,
        mask_ref,
        features_ref,
        act_one_ref,
        middle_ref,
        act_two_ref,
        residual_ref,
        table_ref,
        own_ref,
        taps_ref,
        sem,
    ) = refs
    pixels, channels = features_ref.shape
    wide = jnp.float32
    own_copy = pltpu.make_async_copy(pieces[0], own_ref, sem)
    own_copy.start()
    table_ref[...] = params_ref[...]
    clear_edges(taps_ref, cols)

    def read_input(rows):
        return features_ref[rows, :].astype(wide)

    def read_middle(rows):
        return middle_ref[rows, :]

    height = lax.axis_index("height")
    own_pixels = pixels // count
    seen = RunningStats()
    for place in list(range(1, count)) + [0]:
        if place == 0:
            own_copy.wait()
        piece = (pieces[place] if place else own_ref)[...]
        start = pl.multiple_of((height ^ place) * own_pixels, own_pixels)
        features_ref[pl.ds(start, own_pixels), :] = piece
        seen.add(piece.astype(wide))
    table_ref[0:1, :], table_ref[1:2, :] = seen.finish(pixels)
    seen = RunningStats()

    def keep(rows, value):
        seen.add(value)
        return value

    run_conv(
        taps_ref,
        product_forward(weights_ref.at[0]),
        mask_ref,
        middle_ref,
        activation(read_input, *norm_rows(table_ref, 0), act_one_ref, taps_ref, cols),
        lambda rows, part: part + table_ref[12:13, :],
        keep,
        cols,
    )
    table_ref[2:3, :], table_ref[3:4, :] = seen.finish(pixels)
    seen = RunningStats()
    run_conv(
        taps_ref,
        product_forward(weights_ref.at[1]),
        mask_ref,
        residual_ref,
        activation(read_middle, *norm_rows(table_ref, 1), act_two_ref, taps_ref, cols),
        lambda rows, part: part + (read_input(rows) + table_ref[13:14, :]),
        keep,
        cols,
    )
    table_ref[4:5, :], table_ref[5:6, :] = seen.finish(pixels)


def score_kernel(
    qkv_ref,
    proj_ref,
    residual_ref,
    table_ref,
    id_rows_ref,
    id_cols_ref,
    normed_ref,
    query_ref,
    key_ref,
    value_ref,
    soft_ref,
    out_flip_ref,
    output_ref,
    value_flip_ref,
    *,
    score_scale,
):
    pixels, channels = residual_ref.shape
    own_pixels = output_ref.shape[0]
    wide = jnp.float32
    exponent = score_scale * 1.4426950408889634
    mean, inverse, gain, shift = norm_rows(table_ref, 2)
    scale = inverse * gain
    block = min(QUERY_ROWS, pixels)

    def project(rows, carry):
        normed = ((residual_ref[rows, :] - mean) * scale + shift).astype(jnp.bfloat16)
        normed_ref[rows, :] = normed
        query_ref[rows, :] = (
            jnp.dot(normed, qkv_ref[:, 0:channels], preferred_element_type=wide)
            + table_ref[14:15, :]
        ).astype(jnp.bfloat16)
        key_ref[rows, :] = jnp.dot(
            normed, qkv_ref[:, channels : 2 * channels], preferred_element_type=wide
        ).astype(jnp.bfloat16)
        values = (
            jnp.dot(normed, qkv_ref[:, 2 * channels :], preferred_element_type=wide)
            + table_ref[15:16, :]
        ).astype(jnp.bfloat16)
        value_ref[rows, :] = values
        value_flip_ref[:, rows] = values.T
        return carry

    each_block(pixels, block, project)

    def attend(rows, carry):
        scores = lax.dot_general(
            key_ref[...], query_ref[rows, :], (((1,), (1,)), ((), ())), preferred_element_type=wide
        )
        same = widen(id_rows_ref[...], block) == id_cols_ref[0:1, rows]
        scores = jnp.where(same, scores, masked_score)
        scores = jnp.exp2((scores - jnp.max(scores, axis=0, keepdims=True)) * exponent)
        weights = scores * (1.0 / jnp.sum(scores, axis=0, keepdims=True))
        soft_ref[:, rows] = weights.astype(jnp.bfloat16)
        return carry

    each_block(pixels, block, attend)

    def collect(rows, carry):
        out_flip_ref[rows, :] = jnp.dot(
            value_flip_ref[rows, :], soft_ref[...], preferred_element_type=wide
        ).astype(jnp.bfloat16)
        return carry

    each_block(channels, channels // 2, collect)
    height = lax.axis_index("height")
    own = pl.ds(pl.multiple_of(height * own_pixels, own_pixels), own_pixels)
    output_ref[...] = (
        residual_ref[own, :]
        + lax.dot_general(
            out_flip_ref[:, own],
            proj_ref[...],
            (((0,), (0,)), ((), ())),
            preferred_element_type=wide,
        )
        + table_ref[16:17, :]
    ).astype(jnp.bfloat16)


def own_quarter():
    height = lax.axis_index("height")
    return (height & 1) * 2 + ((height >> 1) & 1)


def send_order(source_ref, targets, axis, share):
    me = lax.axis_index("canvas")
    for step, target in enumerate(targets):
        place = pl.ds(pl.multiple_of((me ^ step) * share, share), share)
        target[...] = source_ref[place, :] if axis == 0 else source_ref[:, place]


def attention_kernel(
    proj_ref,
    normed_ref,
    query_ref,
    key_ref,
    value_ref,
    soft_ref,
    out_flip_ref,
    *refs,
    score_scale,
    count,
):
    pieces, (grad_ref, packed_ref, sums_ref), refs = (
        refs[:count],
        refs[count : count + 3],
        refs[count + 3 :],
    )
    *mixed_refs, mixed_ref, key_flip_ref, back_ref, score_grad_ref, flip_ref, sems = refs
    pixels, channels = normed_ref.shape
    block = min(QUERY_ROWS, pixels)
    wide = jnp.float32
    copies = place_pieces(pieces, grad_ref, sems)
    for copy in copies:
        copy.start()
    quarter = channels // 4
    own = pl.ds(pl.multiple_of(own_quarter() * quarter, quarter), quarter)
    flip_ref[...] = normed_ref[:, own].T
    key_flip_ref[...] = key_ref[...].T
    for copy in copies:
        copy.wait()

    for start in range(0, pixels, block):
        rows = slice(start, start + block)
        back_ref[rows, :] = lax.dot_general(
            grad_ref[rows, :], proj_ref[...], (((1,), (1,)), ((), ())), preferred_element_type=wide
        ).astype(jnp.bfloat16)
    for start in range(0, pixels, block):
        rows = slice(start, start + block)
        weights = soft_ref[:, rows].astype(wide)
        weight_grad = lax.dot_general(
            value_ref[...],
            back_ref[rows, :],
            (((1,), (1,)), ((), ())),
            preferred_element_type=wide,
        )
        dots = jnp.sum(weights * weight_grad, axis=0, keepdims=True)
        score_grad = (weights * (weight_grad - dots)).astype(jnp.bfloat16)
        score_grad_ref[:, rows] = score_grad
        query_grad = jnp.dot(key_flip_ref[...], score_grad, preferred_element_type=wide)
        packed_ref[rows, 0:channels] = (query_grad * score_scale).astype(jnp.bfloat16).T
        packed_ref[rows, 2 * channels :] = jnp.dot(
            soft_ref[rows, :], back_ref[...], preferred_element_type=wide
        ).astype(jnp.bfloat16)
    for start in range(0, pixels, block):
        rows = slice(start, start + block)
        packed_ref[rows, channels : 2 * channels] = (
            jnp.dot(score_grad_ref[rows, :], query_ref[...], preferred_element_type=wide)
            * score_scale
        ).astype(jnp.bfloat16)

    def pack(rows, carry):
        return (
            carry[0] + fold(packed_ref[rows, 0:channels].astype(wide)),
            carry[1] + fold(packed_ref[rows, 2 * channels :].astype(wide)),
            carry[2] + fold(grad_ref[rows, :].astype(wide)),
        )

    zeros = jnp.zeros((8, channels), wide)
    totals = zeros, zeros, zeros
    for start in range(0, pixels, CHUNK):
        totals = pack(pl.ds(start, CHUNK), totals)
    sums_ref[...] = jnp.zeros(sums_ref.shape, wide)
    for row, total in enumerate(totals):
        sums_ref[8 + row : 9 + row, :] = column_total(total)
    mixed_ref[:, 0 : 3 * channels] = jnp.dot(
        flip_ref[...], packed_ref[...], preferred_element_type=wide
    ).astype(jnp.bfloat16)
    mixed_ref[:, 3 * channels :] = jnp.dot(
        out_flip_ref[own, :], grad_ref[...], preferred_element_type=wide
    ).astype(jnp.bfloat16)
    send_order(mixed_ref, mixed_refs, 0, quarter // len(mixed_refs))


def third_kernel(
    qkv_ref,
    grad_ref,
    packed_ref,
    residual_ref,
    table_ref,
    act_two_ref,
    lanes_ref,
    old_sums_ref,
    residual_grad_ref,
    grad_two_ref,
    sums_ref,
    keep_ref,
    send_ref,
    total_ref,
    flip_ref,
    columns_ref,
    part_ref,
    *,
    cols,
):
    pixels, channels = residual_ref.shape
    block = pixels
    wide = jnp.float32
    mean, inverse, gain, shift = norm_rows(table_ref, 2)
    zeros = jnp.zeros((8, channels), wide)

    sums = (zeros, zeros)
    for start in range(0, pixels, block):
        rows = pl.ds(start, block)
        normed_grad = lax.dot_general(
            packed_ref[rows, :], qkv_ref[...], (((1,), (1,)), ((), ())), preferred_element_type=wide
        )
        total_ref[rows, :] = normed_grad
        normed = (residual_ref[rows, :] - mean) * inverse
        sums = sums[0] + fold(normed_grad), sums[1] + fold(normed_grad * normed)
    sums_ref[...] = old_sums_ref[...]
    sums_ref[5:6, :] = column_total(sums[1])
    sums_ref[6:7, :] = column_total(sums[0])
    mean_grad, mean_cross = back_means(sums, gain, pixels)

    def finish(rows, carry):
        normed = (residual_ref[rows, :] - mean) * inverse
        back = inverse * (total_ref[rows, :] * gain - mean_grad - normed * mean_cross)
        total = grad_ref[rows, :].astype(wide) + back
        residual_grad_ref[rows, :] = total
        low = total.astype(jnp.bfloat16)
        grad_two_ref[rows, :] = low
        return carry + fold(low.astype(wide))

    sums_ref[7:8, :] = column_total(each_chunk(pixels, finish, zeros))
    weight_part(act_two_ref, grad_two_ref, lanes_ref, flip_ref, columns_ref, part_ref, cols)
    keep_half(part_ref, 2, 1, keep_ref, send_ref)


def second_kernel(
    total_ref,
    partial_ref,
    middle_ref,
    table_ref,
    act_one_ref,
    lanes_ref,
    old_sums_ref,
    grad_one_ref,
    sums_ref,
    keep_ref,
    send_ref,
    flip_ref,
    columns_ref,
    part_ref,
    *,
    cols,
):
    pixels, channels = middle_ref.shape
    sums = partial_ref[0:8, :], partial_ref[8:16, :]
    back = norm_back(total_ref, sums, lambda rows: middle_ref[rows, :], table_ref, 1)
    sums_ref[...] = old_sums_ref[...]
    sums_ref[2:3, :] = column_total(sums[1])
    sums_ref[3:4, :] = column_total(sums[0])

    def finish(rows, carry):
        low = back(rows).astype(jnp.bfloat16)
        grad_one_ref[rows, :] = low
        return carry + fold(low.astype(jnp.float32))

    zeros = jnp.zeros((8, channels), jnp.float32)
    sums_ref[4:5, :] = column_total(each_chunk(pixels, finish, zeros))
    weight_part(act_one_ref, grad_one_ref, lanes_ref, flip_ref, columns_ref, part_ref, cols)
    keep_half(part_ref, 1, 2, keep_ref, send_ref)


def keep_half(part_ref, near, far, keep_ref, send_ref):
    me = lax.axis_index("canvas")
    rows, width = part_ref.shape[0], keep_ref.shape[1]
    for target_ref, flip in ((keep_ref, 0), (send_ref, near)):
        for slot in range(2):
            owner = me ^ flip ^ (slot * far)
            place = pl.ds(pl.multiple_of(owner * width, width), width)
            target_ref[slot * rows : (slot + 1) * rows, :] = part_ref[:, place]


def begin_kernel(grad_ref, mask_ref, weights_ref, total_ref, taps_ref, *, cols):
    begin_back(grad_ref, weights_ref.at[0], mask_ref, taps_ref, total_ref, cols)


def first_kernel(
    old_total_ref,
    taps_ref,
    features_ref,
    table_ref,
    mask_ref,
    old_sums_ref,
    weights_ref,
    own_ref,
    sums_ref,
    partial_ref,
    total_ref,
    *,
    cols,
):
    def read(rows):
        return features_ref[rows, :].astype(jnp.float32)

    sums = finish_back(
        weights_ref.at[0],
        mask_ref,
        taps_ref,
        total_ref,
        read,
        table_ref,
        0,
        cols,
        old_total_ref,
    )
    partial_ref[0:8, :], partial_ref[8:16, :] = sums
    sums_ref[...] = old_sums_ref[...]
    sums_ref[0:1, :] = column_total(sums[1])
    sums_ref[1:2, :] = column_total(sums[0])
    count = own_ref.shape[0]
    own = pl.ds(pl.multiple_of(lax.axis_index("height") * count, count), count)
    own_ref[...] = total_ref[own, :]


def own_kernel(
    own_ref,
    partial_ref,
    features_ref,
    residual_grad_ref,
    table_ref,
    packed_ref,
    old_qkv,
    old_proj,
    input_grad_ref,
    qkv_hbm,
    proj_hbm,
    qkv_ref,
    proj_ref,
    sems,
):
    copies = spread_quarters([packed_ref], [2], qkv_ref, proj_ref, qkv_hbm, proj_hbm, sems)
    mean, inverse, gain, shift = norm_rows(table_ref, 0)
    pixels = features_ref.shape[0]
    sums = partial_ref[0:8, :], partial_ref[8:16, :]
    mean_grad, mean_cross = back_means(sums, gain, pixels)
    count = own_ref.shape[0]
    own = pl.ds(pl.multiple_of(lax.axis_index("height") * count, count), count)
    normed = (features_ref[own, :].astype(jnp.float32) - mean) * inverse
    back = inverse * (own_ref[...] * gain - mean_grad - normed * mean_cross)
    input_grad_ref[...] = (residual_grad_ref[own, :] + back).astype(jnp.bfloat16)
    for copy in copies:
        copy.wait()


def place_kernel(*refs):
    joints, (qkv_hbm, proj_hbm, packed_ref, qkv_ref, proj_ref, sems) = refs[:-6], refs[-6:]
    share = packed_ref.shape[0] // len(joints)
    me = lax.axis_index("canvas")
    for step, joint in enumerate(joints):
        place = pl.ds(pl.multiple_of((me ^ step) * share, share), share)
        packed_ref[place, :] = joint[...]
    copies = spread_quarters([packed_ref], [0], qkv_ref, proj_ref, qkv_hbm, proj_hbm, sems)
    for copy in copies:
        copy.wait()


def spread_quarters(packed, flips, qkv_ref, proj_ref, qkv_hbm, proj_hbm, sems):
    quarter = packed[0].shape[0]
    inner = qkv_ref.shape[2]
    copies = []
    for index, packed_ref in enumerate(packed):
        owner = own_quarter() ^ flips[index]
        rows = pl.ds(pl.multiple_of(owner * quarter, quarter), quarter)
        qkv_ref[index] = packed_ref[:, 0:inner].astype(jnp.float32)
        proj_ref[index] = packed_ref[:, inner:].astype(jnp.float32)
        for which, (held, target) in enumerate(((qkv_ref, qkv_hbm), (proj_ref, proj_hbm))):
            copy = pltpu.make_async_copy(held.at[index], target.at[rows, :], sems.at[index, which])
            copy.start()
            copies.append(copy)
    return copies


def join_kernel(
    old_qkv, old_proj, chip_ref, both_ref, qkv_hbm, proj_hbm, qkv_ref, proj_ref, sems
):
    copies = spread_quarters(
        [chip_ref, both_ref], [1, 3], qkv_ref, proj_ref, qkv_hbm, proj_hbm, sems
    )
    for copy in copies:
        copy.wait()


def halve_kernel(keep_ref, got_ref, hold_ref, send_ref):
    total = keep_ref[...].astype(jnp.float32) + got_ref[...].astype(jnp.float32)
    rows = hold_ref.shape[0]
    hold_ref[...] = total[0:rows]
    send_ref[...] = total[rows:].astype(jnp.bfloat16)


def sums_kernel(
    sums_ref,
    got_sums_ref,
    hold_one_ref,
    got_one_ref,
    hold_two_ref,
    got_two_ref,
    share_ref,
    gains_ref,
    shifts_ref,
    conv_ref,
    qv_ref,
    proj_ref,
):
    for which, (hold_ref, got_ref) in enumerate(
        ((hold_one_ref, got_one_ref), (hold_two_ref, got_two_ref))
    ):
        total = hold_ref[...] + got_ref[...].astype(jnp.float32)
        share_ref[which] = total.reshape(share_ref.shape[1:])
    total = sums_ref[...] + got_sums_ref[...]
    for row, start in enumerate((0, 2, 5)):
        gains_ref[row : row + 1, :] = total[start : start + 1]
        shifts_ref[row : row + 1, :] = total[start + 1 : start + 2]
    conv_ref[0:1, :] = total[4:5]
    conv_ref[1:2, :] = total[7:8]
    qv_ref[...] = total[8:10]
    proj_ref[...] = total[10:11]


def call_kernel(kernel, outputs, scratch, operands, places, flops, limit, out_places=None, aliases={}):
    out_places = out_places or "v" * len(outputs)
    spaces = {
        "v": pl.BlockSpec(memory_space=pltpu.VMEM),
        "s": pl.BlockSpec(memory_space=pltpu.SMEM),
        "h": pl.BlockSpec(memory_space=pl.ANY),
        "o": pl.BlockSpec(memory_space=pltpu.VMEM),
        "a": pl.BlockSpec(memory_space=pl.ANY),
    }
    moved = 8 * flops // LANES
    held = {"v": pltpu.VMEM, "h": pltpu.HBM, "o": jax.ShapeDtypeStruct}
    operands = [
        pltpu.with_memory_space_constraint(array, pltpu.HBM) if place == "h" else array
        for array, place in zip(operands, places)
    ]
    return pl.pallas_call(
        kernel,
        out_shape=[held[place](*output) for output, place in zip(outputs, out_places)],
        in_specs=[spaces[place] for place in places],
        out_specs=[spaces[place] for place in out_places],
        scratch_shapes=scratch,
        input_output_aliases=aliases,
        compiler_params=pltpu.CompilerParams(vmem_limit_bytes=limit * 2**20),
        cost_estimate=pl.CostEstimate(flops=flops, bytes_accessed=moved, transcendentals=0),
    )(*operands)


def send_height(block, step):
    size = lax.axis_size("height")
    return lax.ppermute(block, "height", [(i, i ^ step) for i in range(size)])


def with_cores(blocks):
    return [piece for block in blocks for piece in (block, send_height(block, 1))]


def send_canvas(block, step):
    size = lax.axis_size("canvas")
    return lax.ppermute(block, "canvas", [(i, i ^ step) for i in range(size)])


def trade_canvas(pieces):
    return [pieces[0]] + [send_canvas(piece, step) for step, piece in enumerate(pieces) if step]


def whole_canvas(
    features,
    tile_ids,
    norm_gains,
    norm_shifts,
    conv_weights,
    conv_biases,
    qkv_weight,
    qv_bias,
    proj_weight,
    proj_bias,
    cotangent,
):
    height_size = lax.axis_size("height")
    canvas_size = lax.axis_size("canvas")
    local_rows, cols, channels = features.shape[1:]
    all_rows = tile_ids.shape[1]
    pixels = all_rows * cols
    own_pixels = local_rows * cols
    out_share = channels // height_size
    ci_share = channels // canvas_size
    quarter = channels // 4
    row_share = quarter // canvas_size
    low, wide = jnp.bfloat16, jnp.float32

    own_features = features.reshape(own_pixels, channels)
    own_grad = cotangent.reshape(own_pixels, channels)
    steps = range(2, height_size, 2)
    held_features = [own_features] + [send_height(own_features, step) for step in steps]
    plane = ((pixels, channels), low)
    plane_wide = ((pixels, channels), wide)
    sums_shape = ((16, channels), wide)
    mixed_shapes = [((row_share, 4 * channels), low)] * canvas_size
    taps = pltpu.VMEM((pixels + 2 * cols, 3 * channels), low)
    held_wide = pltpu.VMEM((pixels, channels), wide)
    flipped = pltpu.VMEM((channels, pixels), low)
    narrow = pltpu.VMEM((NARROW, pixels), low)
    columns = pltpu.VMEM((9 * out_share, pixels), low)
    part_held = pltpu.VMEM((9 * out_share, channels), low)
    sem = pltpu.SemaphoreType.DMA
    conv_flops = 2 * 9 * pixels * channels * channels
    dot_flops = 2 * pixels * channels * channels
    score_flops = 2 * pixels * pixels * channels
    scale = channels ** (-0.5)

    (
        held_conv,
        turned,
        held_qkv,
        held_proj,
        params,
        mask,
        lane_mask,
        id_rows,
        id_cols,
    ) = call_kernel(
        functools.partial(hold_kernel, cols=cols),
        [
            (conv_weights.shape, low),
            ((2, 3, channels, 3 * channels), low),
            (qkv_weight.shape, low),
            (proj_weight.shape, low),
            ((24, channels), wide),
            ((2, pixels, LANES), wide),
            ((8, pixels), wide),
            ((pixels, LANES), jnp.int32),
            ((8, pixels), jnp.int32),
        ],
        [
            pltpu.SMEM(tile_ids.shape, jnp.int32),
            pltpu.VMEM(norm_gains.shape, wide),
            pltpu.VMEM(norm_shifts.shape, wide),
            pltpu.VMEM(conv_biases.shape, wide),
            pltpu.VMEM(qv_bias.shape, wide),
            pltpu.VMEM((1, channels), wide),
            sem((27,)),
        ],
        [
            tile_ids,
            norm_gains,
            norm_shifts,
            conv_biases,
            conv_weights,
            qkv_weight,
            proj_weight,
            qv_bias,
            proj_bias.reshape(1, channels),
        ],
        "h" * 9,
        conv_flops,
        8,
    )
    held_features[1:] = [
        lax.optimization_barrier((params, block))[1] for block in held_features[1:]
    ]
    pieces = with_cores(held_features)
    far_grad, *pieces[4::2] = lax.optimization_barrier((own_grad, *held_features[2:]))
    held_grads = [own_grad, send_height(own_grad, 2)]
    held_grads[1], pieces[2] = lax.optimization_barrier((held_grads[1], held_features[1]))
    held_grads += [send_height(far_grad, step) for step in steps[1:]]

    all_features, act_one, middle, act_two, residual, table = call_kernel(
        functools.partial(conv_kernel, cols=cols, count=height_size),
        [plane, plane, plane_wide, plane, plane_wide, ((24, channels), wide)],
        [pltpu.VMEM((own_pixels, channels), low), taps, sem],
        [*pieces, held_conv, params, mask],
        "h" + "v" * (height_size + 2),
        2 * conv_flops,
        16,
    )
    residual, *held_grads = lax.optimization_barrier((residual, *held_grads))
    grad_pieces = with_cores(held_grads)
    normed, query, key, value, soft, out_flip, output = call_kernel(
        functools.partial(score_kernel, score_scale=scale),
        [
            plane,
            plane,
            plane,
            plane,
            ((pixels, pixels), low),
            ((channels, pixels), low),
            ((own_pixels, channels), low),
        ],
        [
            flipped,
        ],
        [
            held_qkv,
            held_proj,
            residual,
            table,
            id_rows,
            id_cols,
        ],
        "vvvvvv",
        3 * dot_flops + 2 * score_flops,
        16,
        "v" * 6 + "o",
    )
    normed, *grad_pieces = lax.optimization_barrier((normed, *grad_pieces))
    all_grad, packed, sums, *mixed = call_kernel(
        functools.partial(attention_kernel, score_scale=scale, count=height_size),
        [plane, ((pixels, 3 * channels), low), sums_shape, *mixed_shapes],
        [
            pltpu.VMEM((quarter, 4 * channels), low),
            flipped,
            pltpu.VMEM((pixels, channels), low),
            pltpu.VMEM((pixels, pixels), low),
            pltpu.VMEM((quarter, pixels), low),
            sem((height_size,)),
        ],
        [held_proj, normed, query, key, value, soft, out_flip, *grad_pieces],
        "vvvvvvvh" + "a" * (height_size - 1),
        3 * dot_flops + 4 * score_flops,
        20,
    )
    mixed = trade_canvas(mixed)
    halves = [((18 * out_share, ci_share), low)] * 2
    residual_grad, grad_two, sums, keep_two, send_two = call_kernel(
        functools.partial(third_kernel, cols=cols),
        [plane_wide, plane, sums_shape, *halves],
        [held_wide, narrow, columns, part_held],
        [held_qkv, all_grad, packed, residual, table, act_two, lane_mask, sums],
        "vvvvvvvv",
        3 * dot_flops + conv_flops // height_size,
        16,
    )
    grad_two, *mixed = lax.optimization_barrier((grad_two, *mixed))
    mixed_sum = mixed[0].astype(wide)
    for piece in mixed[1:]:
        mixed_sum = mixed_sum + piece.astype(wide)
    joints = trade_canvas([mixed_sum.astype(low)] * canvas_size)
    act_two_grad, partial_sums = call_kernel(
        functools.partial(turn_kernel, cols=cols),
        [plane_wide, sums_shape],
        [taps],
        [grad_two, mask, turned, middle, table],
        "vvvvv",
        conv_flops,
        16,
    )
    act_two_grad, *joints = lax.optimization_barrier((act_two_grad, *joints))
    qkv_grad, proj_grad, own_mixed = call_kernel(
        place_kernel,
        [(qkv_weight.shape, wide), (proj_weight.shape, wide), ((quarter, 4 * channels), low)],
        [
            pltpu.VMEM((1, quarter, 3 * channels), wide),
            pltpu.VMEM((1, quarter, channels), wide),
            sem((1, 2)),
        ],
        joints,
        "v" * canvas_size,
        0,
        12,
        "hhv",
    )
    own_mixed, send_two = lax.optimization_barrier((own_mixed, send_two))
    got_two = send_canvas(send_two, 2)
    chip_mixed = send_height(own_mixed, 2)
    core_mixed = send_height(own_mixed, 1)
    grad_one, sums, keep_one, send_one = call_kernel(
        functools.partial(second_kernel, cols=cols),
        [plane, sums_shape, *halves],
        [narrow, columns, part_held],
        [act_two_grad, partial_sums, middle, table, act_one, lane_mask, sums],
        "vvvvvvv",
        1,
        16,
    )
    got_one = send_canvas(send_one, 1)

    def halve(keep, got):
        return call_kernel(
            halve_kernel,
            [((9 * out_share, ci_share), kind) for kind in (wide, low)],
            [],
            [keep, got],
            "vv",
            0,
            12,
        )

    half_total, half_taps = call_kernel(
        functools.partial(begin_kernel, cols=cols),
        [plane_wide, (taps.shape, low)],
        [],
        [grad_one, mask, turned],
        "vvv",
        1,
        16,
    )
    half_total, got_two = lax.optimization_barrier((half_total, got_two))
    hold_two, send_two = halve(keep_two, got_two)
    got_two = send_canvas(send_two, 1)
    half_total, hold_two = lax.optimization_barrier((half_total, hold_two))
    own_total, sums, partial_sums = call_kernel(
        functools.partial(first_kernel, cols=cols),
        [((own_pixels, channels), wide), sums_shape, sums_shape],
        [held_wide],
        [half_total, half_taps, all_features, table, mask, sums, turned],
        "vvvvvvv",
        conv_flops // 3,
        16,
    )
    sums, core_mixed, got_one = lax.optimization_barrier((sums, core_mixed, got_one))
    got_sums = send_canvas(sums, 1)
    hold_one, send_one = halve(keep_one, got_one)
    got_one = send_canvas(send_one, 2)
    own_total, hold_one, got_two = lax.optimization_barrier((own_total, hold_one, got_two))
    quarter_scratch = [
        pltpu.VMEM((2, quarter, 3 * channels), wide),
        pltpu.VMEM((2, quarter, channels), wide),
        sem((2, 2)),
    ]
    grad_shapes = [(qkv_weight.shape, wide), (proj_weight.shape, wide)]
    input_grad, qkv_grad, proj_grad = call_kernel(
        own_kernel,
        [((own_pixels, channels), low), *grad_shapes],
        quarter_scratch,
        [
            own_total,
            partial_sums,
            all_features,
            residual_grad,
            table,
            core_mixed,
            qkv_grad,
            proj_grad,
        ],
        "vvvvvvhh",
        1,
        12,
        "ohh",
        {6: 1, 7: 2},
    )
    input_grad, got_sums, chip_mixed = lax.optimization_barrier((input_grad, got_sums, chip_mixed))
    both_mixed = send_height(chip_mixed, 1)
    sums = sums + got_sums
    got_sums = send_canvas(sums, 2)
    both_mixed, got_one, got_two = lax.optimization_barrier((both_mixed, got_one, got_two))
    qkv_grad, proj_grad = call_kernel(
        join_kernel,
        grad_shapes,
        quarter_scratch,
        [qkv_grad, proj_grad, chip_mixed, both_mixed],
        "hhvv",
        0,
        12,
        "hh",
        {0: 0, 1: 1},
    )
    qkv_grad, got_sums = lax.optimization_barrier((qkv_grad, got_sums))
    vector_shapes = [norm_gains.shape, norm_shifts.shape, conv_biases.shape, qv_bias.shape]
    conv_grad, gains_grad, shifts_grad, biases_grad, qv_grad, proj_bias_grad = call_kernel(
        sums_kernel,
        [((2, 3, 3, out_share, ci_share), wide)]
        + [(shape, wide) for shape in vector_shapes + [(1, channels)]],
        [],
        [sums, got_sums, hold_one, got_one, hold_two, got_two],
        "vvvvvv",
        0,
        12,
        "o" * 6,
    )
    own_shape = (1, local_rows, cols, channels)
    return (
        output.reshape(own_shape),
        input_grad.reshape(own_shape),
        gains_grad,
        shifts_grad,
        jnp.swapaxes(conv_grad, 3, 4),
        biases_grad,
        qkv_grad,
        qv_grad,
        proj_grad,
        proj_bias_grad.reshape(channels),
    )


def on_device(*arrays):
    features, tile_ids = arrays[0], arrays[1]
    local_rows, cols, channels = features.shape[1:]
    pixels = tile_ids.shape[1] * cols
    height_size, canvas_size = lax.axis_size("height"), lax.axis_size("canvas")
    powers = all(size & (size - 1) == 0 for size in (height_size, canvas_size, cols))
    fits = (
        powers
        and height_size > 2
        and canvas_size == 4
        and channels == LANES * canvas_size
        and pixels <= MOST_PIXELS
        and pixels % FILL_ROWS == 0
        and FILL_ROWS % CHUNK == 0
        and pixels % KEY_ROWS == 0
        and (local_rows * cols) % LANES == 0
        and CHUNK % cols == 0
        and cols % 16 == 0
        and channels % (LANES * canvas_size) == 0
        and 2 * channels == NARROW * height_size
    )
    return whole_canvas(*arrays) if fits else split_canvas(*arrays)


def solution(mesh):
    in_specs = (
        P("canvas", "height", None, None),
        P("canvas", None),
        P(),
        P(),
        P(),
        P(),
        P(),
        P(),
        P(),
        P(),
        P("canvas", "height", None, None),
    )
    out_specs = (
        P("canvas", "height", None, None),
        P("canvas", "height", None, None),
        P(),
        P(),
        P(None, None, None, "canvas", "height"),
        P(),
        P(),
        P(),
        P(),
        P(),
    )
    return jax.shard_map(
        on_device, mesh=mesh, in_specs=in_specs, out_specs=out_specs, check_vma=False
    )
```

```python
import functools

import jax
import jax.numpy as jnp
from jax import lax
from jax.experimental import pallas as pl
from jax.experimental.pallas import tpu as pltpu
from jax.sharding import PartitionSpec as P

GROUPS = 32


epsilon = 1e-06
masked_score = -1e30
MOST_PIXELS = 1024
LANES = 128
NARROW = 128
CHUNK = 128
CONV_ROWS = 1024
FILL_ROWS = 256
QUERY_ROWS = 512
KEY_ROWS = 256


def extended(block, sides, width):
    for axis, dim in sides:
        count = lax.axis_size(axis)
        forward = [(i, i + 1) for i in range(count - 1)]
        backward = [(target, source) for source, target in forward]
        low = lax.ppermute(
            lax.slice_in_dim(block, block.shape[dim] - width, None, axis=dim), axis, forward
        )
        high = lax.ppermute(lax.slice_in_dim(block, 0, width, axis=dim), axis, backward)
        block = jnp.concatenate([low, block, high], axis=dim)
    return block


def group_total(vector):
    return vector.reshape(GROUPS, -1).sum(axis=1)


def spread_groups(vector, channels):
    return jnp.repeat(vector, channels // GROUPS)


def norm_forward(values, gain, shift, members):
    channels = values.shape[1]
    totals = lax.psum(group_total(jnp.sum(values, axis=0)), "height")
    centered = values - spread_groups(totals / members, channels)
    squares = lax.psum(group_total(jnp.sum(centered * centered, axis=0)), "height")
    inverse = spread_groups(lax.rsqrt(squares / members + epsilon), channels)
    normed = centered * inverse
    return (normed, inverse, normed * gain + shift)


def norm_backward(grad_in, normed, inverse, gain, members):
    channels = grad_in.shape[1]
    scaled = grad_in * gain
    both_sums = lax.psum(
        (group_total(jnp.sum(scaled, axis=0)), group_total(jnp.sum(scaled * normed, axis=0))),
        "height",
    )
    mean_grad = spread_groups(both_sums[0] / members, channels)
    mean_cross = spread_groups(both_sums[1] / members, channels)
    result = inverse * (scaled - mean_grad - normed * mean_cross)
    return (result, jnp.sum(grad_in * normed, axis=0), jnp.sum(grad_in, axis=0))


def swish(values):
    return values * jax.nn.sigmoid(values)


def swish_slope(values):
    sigmoid_part = jax.nn.sigmoid(values)
    return sigmoid_part * (1.0 + values * (1.0 - sigmoid_part))


def tap_columns(padded, row_mask, local_rows, canvas_cols):
    pieces = []
    for row_tap in range(3):
        rows_taken = padded[row_tap : row_tap + local_rows] * row_mask[:, row_tap, None, None]
        for col_tap in range(3):
            pieces.append(rows_taken[:, col_tap : col_tap + canvas_cols])
    stacked = jnp.concatenate(pieces, axis=2)
    return stacked.reshape(local_rows * canvas_cols, stacked.shape[2])


def conv_forward(acts, row_mask, weight, bias):
    local_rows, canvas_cols, channels = acts.shape
    rimmed = extended(acts, (("height", 0),), 1)
    padded = jnp.pad(rimmed, ((0, 0), (1, 1), (0, 0)))
    gathered = tap_columns(padded, row_mask, local_rows, canvas_cols)
    result = (
        jnp.dot(
            gathered, weight.reshape(9 * channels, channels), preferred_element_type=jnp.float32
        )
        + bias
    )
    return (result, gathered)


def conv_backward(grad_low, row_mask, weight, gathered):
    local_rows, canvas_cols, channels = grad_low.shape
    flat_grad = grad_low.reshape(local_rows * canvas_cols, channels)
    weight_grad = lax.dot_general(
        gathered, flat_grad, (((0,), (0,)), ((), ())), preferred_element_type=jnp.float32
    )
    rimmed = extended(grad_low, (("height", 0),), 1)
    padded = jnp.pad(rimmed, ((0, 0), (1, 1), (0, 0)))
    grad_taps = tap_columns(padded, row_mask, local_rows, canvas_cols)
    flipped = jnp.transpose(weight[::-1, ::-1], (0, 1, 3, 2)).reshape(9 * channels, channels)
    input_part = jnp.dot(grad_taps, flipped, preferred_element_type=jnp.float32)
    return (
        input_part,
        weight_grad.reshape(3, 3, channels, channels),
        jnp.sum(flat_grad.astype(jnp.float32), axis=0),
    )


def take_rows(array, offset, count):
    return lax.dynamic_slice_in_dim(array, offset, count)


def score_grads(
    queries, out_grad, log_total, row_dots, query_ids, key_rows, value_rows, key_ids, score_scale
):
    scores = (
        lax.dot_general(
            queries, key_rows, (((1,), (1,)), ((), ())), preferred_element_type=jnp.float32
        )
        * score_scale
    )
    same_tile = query_ids[:, None] == key_ids[None, :]
    softmax_block = jnp.exp(jnp.where(same_tile, scores - log_total[:, None], masked_score))
    weight_grad = lax.dot_general(
        out_grad, value_rows, (((1,), (1,)), ((), ())), preferred_element_type=jnp.float32
    )
    score_grad = (softmax_block * (weight_grad - row_dots[:, None])).astype(jnp.bfloat16)
    return (softmax_block.astype(jnp.bfloat16), score_grad)


def split_canvas(
    features,
    tile_ids,
    norm_gains,
    norm_shifts,
    conv_weights,
    conv_biases,
    qkv_weight,
    qv_bias,
    proj_weight,
    proj_bias,
    cotangent,
):
    height_size = lax.axis_size("height")
    local_rows = features.shape[1]
    canvas_cols = features.shape[2]
    channels = features.shape[3]
    pixels = local_rows * canvas_cols
    row_ids = tile_ids[0]
    all_rows = row_ids.shape[0]
    members = float(all_rows * canvas_cols * (channels // GROUPS))
    score_scale = channels ** (-0.5)
    first_row = lax.axis_index("height") * local_rows
    edge_ids = jnp.full((1,), -1, jnp.int32)
    padded_ids = jnp.concatenate([edge_ids, row_ids, edge_ids])
    near_ids = lax.dynamic_slice_in_dim(padded_ids, first_row, local_rows + 2)
    own_rows = near_ids[1 : local_rows + 1]
    row_mask = jnp.stack(
        [near_ids[row_tap : row_tap + local_rows] == own_rows for row_tap in range(3)], axis=1
    ).astype(jnp.bfloat16)
    key_ids = jnp.repeat(row_ids, canvas_cols)
    query_ids = jnp.repeat(own_rows, canvas_cols)
    grid_shape = (local_rows, canvas_cols, channels)
    inputs = features[0].reshape(pixels, channels).astype(jnp.float32)
    normed_one, inverse_one, pre_one = norm_forward(inputs, norm_gains[0], norm_shifts[0], members)
    act_one = swish(pre_one).astype(jnp.bfloat16).reshape(grid_shape)
    middle, taps_one = conv_forward(act_one, row_mask, conv_weights[0], conv_biases[0])
    normed_two, inverse_two, pre_two = norm_forward(middle, norm_gains[1], norm_shifts[1], members)
    act_two = swish(pre_two).astype(jnp.bfloat16).reshape(grid_shape)
    branch, taps_two = conv_forward(act_two, row_mask, conv_weights[1], conv_biases[1])
    residual = inputs + branch
    normed_three, inverse_three, pre_three = norm_forward(
        residual, norm_gains[2], norm_shifts[2], members
    )
    attn_input = pre_three.astype(jnp.bfloat16)
    mixed = jnp.dot(attn_input, qkv_weight, preferred_element_type=jnp.float32)
    queries = (mixed[:, :channels] + qv_bias[0]).astype(jnp.bfloat16)
    key_rows = mixed[:, channels : 2 * channels].astype(jnp.bfloat16)
    value_rows = (mixed[:, 2 * channels :] + qv_bias[1]).astype(jnp.bfloat16)
    running_max = jnp.full((pixels,), masked_score, jnp.float32)
    key_piece = lax.all_gather(key_rows, "height", axis=0, tiled=True)
    value_piece = lax.all_gather(value_rows, "height", axis=0, tiled=True)
    scores = (
        lax.dot_general(
            queries, key_piece, (((1,), (1,)), ((), ())), preferred_element_type=jnp.float32
        )
        * score_scale
    )
    same_tile = query_ids[:, None] == key_ids[None, :]
    scores = jnp.where(same_tile, scores, masked_score)
    new_max = jnp.maximum(running_max, jnp.max(scores, axis=1))
    weights = jnp.where(same_tile, jnp.exp(scores - new_max[:, None]), 0.0)
    summed_out = jnp.dot(
        weights.astype(jnp.bfloat16), value_piece, preferred_element_type=jnp.float32
    )
    total_weight = jnp.sum(weights, axis=1)
    log_total = new_max + jnp.log(total_weight)
    attended = summed_out / total_weight[:, None]
    attended_low = attended.astype(jnp.bfloat16)
    output = (
        residual
        + jnp.dot(attended_low, proj_weight, preferred_element_type=jnp.float32)
        + proj_bias
    )
    out_grad = cotangent[0].reshape(pixels, channels)
    out_grad_full = out_grad.astype(jnp.float32)
    proj_grad = lax.dot_general(
        attended_low, out_grad, (((0,), (0,)), ((), ())), preferred_element_type=jnp.float32
    )
    proj_bias_grad = jnp.sum(out_grad_full, axis=0)
    attended_grad = lax.dot_general(
        out_grad, proj_weight, (((1,), (1,)), ((), ())), preferred_element_type=jnp.float32
    ).astype(jnp.bfloat16)
    row_dots = jnp.sum(attended_grad.astype(jnp.float32) * attended, axis=1)
    block_rows = pixels * min(height_size, 8)
    zero_block = jnp.zeros((pixels, channels), jnp.float32)
    key_all, value_all = (
        lax.all_gather(key_rows, "height", axis=0, tiled=True),
        lax.all_gather(value_rows, "height", axis=0, tiled=True),
    )
    query_all, grad_all = (
        lax.all_gather(queries, "height", axis=0, tiled=True),
        lax.all_gather(attended_grad, "height", axis=0, tiled=True),
    )
    total_all, dots_all = (
        lax.all_gather(log_total, "height", axis=0, tiled=True),
        lax.all_gather(row_dots, "height", axis=0, tiled=True),
    )

    def own_query_step(running, block_index):
        offset = block_index * block_rows
        key_part = take_rows(key_all, offset, block_rows)
        rounded, score_grad = score_grads(
            queries,
            attended_grad,
            log_total,
            row_dots,
            query_ids,
            key_part,
            take_rows(value_all, offset, block_rows),
            take_rows(key_ids, offset, block_rows),
            score_scale,
        )
        return (
            running
            + jnp.dot(score_grad, key_part, preferred_element_type=jnp.float32) * score_scale,
            None,
        )

    def own_key_step(running, block_index):
        offset = block_index * block_rows
        query_part = take_rows(query_all, offset, block_rows)
        grad_part = take_rows(grad_all, offset, block_rows)
        rounded, score_grad = score_grads(
            query_part,
            grad_part,
            take_rows(total_all, offset, block_rows),
            take_rows(dots_all, offset, block_rows),
            take_rows(key_ids, offset, block_rows),
            key_rows,
            value_rows,
            query_ids,
            score_scale,
        )
        key_part = (
            lax.dot_general(
                score_grad, query_part, (((0,), (0,)), ((), ())), preferred_element_type=jnp.float32
            )
            * score_scale
        )
        value_part = lax.dot_general(
            rounded, grad_part, (((0,), (0,)), ((), ())), preferred_element_type=jnp.float32
        )
        return ((running[0] + key_part, running[1] + value_part), None)

    block_count = key_all.shape[0] // block_rows
    query_grad, unused_one = lax.scan(own_query_step, zero_block, jnp.arange(block_count))
    (key_grad, value_grad), unused_two = lax.scan(
        own_key_step, (zero_block, zero_block), jnp.arange(block_count)
    )
    query_low = query_grad.astype(jnp.bfloat16)
    key_low = key_grad.astype(jnp.bfloat16)
    value_low = value_grad.astype(jnp.bfloat16)
    stacked_grad = jnp.concatenate([query_low, key_low, value_low], axis=1)
    qkv_grad = lax.dot_general(
        attn_input, stacked_grad, (((0,), (0,)), ((), ())), preferred_element_type=jnp.float32
    )
    qv_grad = jnp.stack(
        [
            jnp.sum(query_low.astype(jnp.float32), axis=0),
            jnp.sum(value_low.astype(jnp.float32), axis=0),
        ]
    )
    normed_grad = lax.dot_general(
        stacked_grad, qkv_weight, (((1,), (1,)), ((), ())), preferred_element_type=jnp.float32
    )
    back_three, gain_three, shift_three = norm_backward(
        normed_grad, normed_three, inverse_three, norm_gains[2], members
    )
    residual_grad = out_grad_full + back_three
    grad_two = residual_grad.astype(jnp.bfloat16).reshape(grid_shape)
    act_two_grad, weight_two_grad, bias_two_grad = conv_backward(
        grad_two, row_mask, conv_weights[1], taps_two
    )
    middle_grad, gain_two, shift_two = norm_backward(
        act_two_grad * swish_slope(pre_two), normed_two, inverse_two, norm_gains[1], members
    )
    grad_one = middle_grad.astype(jnp.bfloat16).reshape(grid_shape)
    act_one_grad, weight_one_grad, bias_one_grad = conv_backward(
        grad_one, row_mask, conv_weights[0], taps_one
    )
    input_back, gain_one, shift_one = norm_backward(
        act_one_grad * swish_slope(pre_one), normed_one, inverse_one, norm_gains[0], members
    )
    input_grad = residual_grad + input_back
    conv_grad = jnp.stack([weight_one_grad, weight_two_grad])
    conv_part = lax.psum_scatter(conv_grad, "height", scatter_dimension=4, tiled=True)
    conv_part = lax.psum_scatter(
        conv_part.astype(jnp.bfloat16), "canvas", scatter_dimension=3, tiled=True
    ).astype(jnp.float32)
    summed = lax.psum(
        (
            jnp.stack([gain_one, gain_two, gain_three]),
            jnp.stack([shift_one, shift_two, shift_three]),
            jnp.stack([bias_one_grad, bias_two_grad]),
            qkv_grad,
            qv_grad,
            proj_grad,
            proj_bias_grad,
        ),
        ("canvas", "height"),
    )
    return (
        output.astype(jnp.bfloat16).reshape((1,) + grid_shape),
        input_grad.astype(jnp.bfloat16).reshape((1,) + grid_shape),
        summed[0],
        summed[1],
        conv_part,
        summed[2],
        summed[3],
        summed[4],
        summed[5],
        summed[6],
    )


def fold(block):
    rows, width = block.shape
    return jnp.sum(block.reshape(rows // 8, 8, width), axis=0)


def group_lanes(block, group):
    lane = lax.broadcasted_iota(jnp.int32, block.shape, 1)
    width = block.shape[1]
    step = 1
    while step < group:
        above = pltpu.roll(block, step, 1)
        below = pltpu.roll(block, width - step, 1)
        block = block + jnp.where((lane & step) != 0, above, below)
        step *= 2
    return block


def group_mean(partial, members):
    spread = group_lanes(partial, partial.shape[1] // GROUPS)
    return jnp.sum(spread, axis=0, keepdims=True) * (1.0 / members)


def widen(block, width):
    return jnp.concatenate([block] * (width // block.shape[1]), axis=1)


def each_block(pixels, block, body, carry=0):
    def step(index, carry):
        return body(pl.ds(pl.multiple_of(index * block, block), block), carry)

    return lax.fori_loop(0, pixels // block, step, carry)


def each_chunk(pixels, body, carry):
    return each_block(pixels, CHUNK, body, carry)


def aligned(start, step):
    return start if isinstance(start, int) else pl.multiple_of(start, step)


def fold_about(block, center):
    rows, width = block.shape
    offset = block.reshape(rows // 8, 8, width) - center[None]
    return jnp.sum(offset, axis=0), jnp.sum(offset * offset, axis=0)


def finish_stats(center, sums, squares, pixels):
    width = center.shape[1] // GROUPS
    share = pixels / 8.0
    means = center + sums * (1.0 / share)
    spread = squares - sums * sums * (1.0 / share)
    mean = group_mean(means, 8.0 * width)
    offset = means - mean
    variance = group_mean(spread + share * offset * offset, float(pixels * width))
    return mean, lax.rsqrt(variance + epsilon)


class RunningStats:
    def __init__(self):
        self.center = None

    def add(self, block):
        if self.center is None:
            self.center = block[0:8]
            self.sums, self.squares = fold_about(block, self.center)
        else:
            sums, squares = fold_about(block, self.center)
            self.sums, self.squares = self.sums + sums, self.squares + squares

    def finish(self, pixels):
        return finish_stats(self.center, self.sums, self.squares, pixels)


def put_taps(taps_ref, block, rows, cols):
    count, channels = block.shape
    place = lax.broadcasted_iota(jnp.int32, block.shape, 0) & (cols - 1)
    left = jnp.where(place == 0, 0.0, pltpu.roll(block, 1, 0))
    right = jnp.where(place == cols - 1, 0.0, pltpu.roll(block, count - 1, 0))
    inner = pl.ds(aligned(rows.start + cols, cols), count)
    taps_ref[inner, 0:channels] = left.astype(jnp.bfloat16)
    taps_ref[inner, channels : 2 * channels] = block.astype(jnp.bfloat16)
    taps_ref[inner, 2 * channels :] = right.astype(jnp.bfloat16)


def clear_edges(taps_ref, cols):
    edge = jnp.zeros((cols, taps_ref.shape[1]), taps_ref.dtype)
    taps_ref[0:cols, :] = edge
    taps_ref[taps_ref.shape[0] - cols :, :] = edge


def begin_conv(taps_ref, product, total_ref, fill, first, cols):
    for start in range(0, total_ref.shape[0], FILL_ROWS):
        for inner in range(start, start + FILL_ROWS, CHUNK):
            fill(pl.ds(inner, CHUNK))
        rows = pl.ds(start, FILL_ROWS)
        total_ref[rows, :] = first(rows, product(taps_ref, pl.ds(start + cols, FILL_ROWS), 1))


def add_rows(taps_ref, product, mask_ref, total_ref, row_tap, last, cols, old_ref=None):
    pixels, channels = total_ref.shape
    rows = pl.ds(0, pixels)
    part = product(taps_ref, pl.ds(row_tap * cols, pixels), row_tap)
    old_ref = total_ref if old_ref is None else old_ref
    value = old_ref[...] + widen(mask_ref[row_tap // 2], channels) * part
    total_ref[...] = last(rows, value)


def run_conv(taps_ref, product, mask_ref, total_ref, fill, first, last, cols):
    begin_conv(taps_ref, product, total_ref, fill, first, cols)
    add_rows(taps_ref, product, mask_ref, total_ref, 0, lambda rows, value: value, cols)
    add_rows(taps_ref, product, mask_ref, total_ref, 2, last, cols)


def product_forward(weight_ref):
    channels = weight_ref.shape[-1]

    def product(taps_ref, shifted, row_tap):
        return jnp.dot(
            taps_ref[shifted, :],
            weight_ref[row_tap].reshape(3 * channels, channels),
            preferred_element_type=jnp.float32,
        )

    return product


def product_backward(weight_ref):
    def product(taps_ref, shifted, row_tap):
        return lax.dot_general(
            taps_ref[shifted, :],
            weight_ref[row_tap],
            (((1,), (1,)), ((), ())),
            preferred_element_type=jnp.float32,
        )

    return product


def smooth(values):
    part = 0.5 * jnp.tanh(0.5 * values) + 0.5
    return values * part, part


def activation(read, mean, inverse, gain, shift, act_ref, taps_ref, cols):
    scale = inverse * gain

    def fill(rows):
        act = smooth((read(rows) - mean) * scale + shift)[0]
        act_ref[rows, :] = act.astype(jnp.bfloat16)
        put_taps(taps_ref, act, rows, cols)

    return fill


def back_means(sums, gain, pixels):
    channels = gain.shape[1]
    members = float(pixels * (channels // GROUPS))
    return group_mean(sums[0] * gain, members), group_mean(sums[1] * gain, members)


def column_total(partial):
    return jnp.sum(partial, axis=0, keepdims=True)


def weight_part(act_ref, grad_ref, lanes_ref, flip_ref, columns_ref, part_ref, cols):
    pixels, channels = act_ref.shape
    height = lax.axis_index("height")
    share = NARROW // 2
    block = pl.ds(pl.multiple_of((height // 2) * NARROW, NARROW), NARROW)
    flip_ref[...] = grad_ref[:, block].T
    own = pl.ds(pl.multiple_of((height % 2) * share, share), share)
    grad = flip_ref[own, :].astype(jnp.float32)
    column = lax.broadcasted_iota(jnp.int32, grad.shape, 1) & (cols - 1)
    for col_tap in range(3):
        shifted = grad
        if col_tap == 0:
            shifted = jnp.where(column == cols - 1, 0.0, pltpu.roll(grad, pixels - 1, 1))
        elif col_tap == 2:
            shifted = jnp.where(column == 0, 0.0, pltpu.roll(grad, 1, 1))
        for row_tap in range(3):
            tap = 3 * row_tap + col_tap
            place = slice(tap * share, (tap + 1) * share)
            if row_tap == 1:
                columns_ref[place, :] = shifted.astype(jnp.bfloat16)
                continue
            side, turn = (0, pixels - cols) if row_tap == 0 else (1, cols)
            masked = (shifted * lanes_ref[side : side + 1, :]).astype(jnp.bfloat16)
            columns_ref[place, :] = pltpu.roll(masked, turn, 1)
    part_ref[...] = jnp.dot(
        columns_ref[...], act_ref[...], preferred_element_type=jnp.float32
    ).astype(jnp.bfloat16)


def begin_back(grad_ref, weights_ref, mask_ref, taps_ref, total_ref, cols):
    clear_edges(taps_ref, cols)

    def fill(rows):
        put_taps(taps_ref, grad_ref[rows, :].astype(jnp.float32), rows, cols)

    product = product_backward(weights_ref)
    begin_conv(taps_ref, product, total_ref, fill, lambda rows, part: part, cols)
    add_rows(taps_ref, product, mask_ref, total_ref, 0, lambda rows, value: value, cols)


def finish_back(
    weights_ref, mask_ref, taps_ref, total_ref, read, table_ref, which, cols, old_ref=None
):
    mean, inverse, gain, shift = norm_rows(table_ref, which)
    sums = []

    def slope(rows, value):
        normed = (read(rows) - mean) * inverse
        pre = normed * gain + shift
        part = smooth(pre)[1]
        grad = value * (part * (1.0 + pre * (1.0 - part)))
        sums.append((fold(grad), fold(grad * normed)))
        return grad

    add_rows(
        taps_ref, product_backward(weights_ref), mask_ref, total_ref, 2, slope, cols, old_ref
    )
    return sums[0]


def norm_back(total_ref, sums, read, table_ref, which):
    mean, inverse, gain, shift = norm_rows(table_ref, which)
    mean_grad, mean_cross = back_means(sums, gain, total_ref.shape[0])

    def back(rows):
        normed = (read(rows) - mean) * inverse
        return inverse * (total_ref[rows, :] * gain - mean_grad - normed * mean_cross)

    return back


def turn_kernel(
    grad_ref, mask_ref, weights_ref, middle_ref, table_ref, total_ref, sums_ref, taps_ref, *, cols
):
    begin_back(grad_ref, weights_ref.at[1], mask_ref, taps_ref, total_ref, cols)
    sums_ref[0:8, :], sums_ref[8:16, :] = finish_back(
        weights_ref.at[1],
        mask_ref,
        taps_ref,
        total_ref,
        lambda rows: middle_ref[rows, :],
        table_ref,
        1,
        cols,
    )


def norm_rows(table_ref, which):
    picks = (2 * which, 2 * which + 1, 6 + which, 9 + which)
    return tuple(table_ref[pick : pick + 1, :] for pick in picks)


def build_masks(ids_ref, mask_ref, lanes_ref, id_rows_ref, id_cols_ref, cols):
    rows = ids_ref.shape[1]
    for row in range(rows):
        here = ids_ref[0, row]
        place = slice(row * cols, (row + 1) * cols)
        id_rows_ref[place, :] = jnp.full((cols, LANES), here, jnp.int32)
        for side, other in ((0, row - 1), (1, row + 1)):
            same = jnp.float32(0.0)
            if 0 <= other < rows:
                same = jnp.where(ids_ref[0, other] == here, 1.0, 0.0).astype(jnp.float32)
            mask_ref[side, place, :] = jnp.full((cols, LANES), same, jnp.float32)
    lane = lax.broadcasted_iota(jnp.int32, (8, LANES), 1)
    each = LANES // cols
    for block in range(rows // each):
        ids = jnp.full((8, LANES), ids_ref[0, block * each], jnp.int32)
        for step in range(1, each):
            ids = jnp.where(lane >= step * cols, ids_ref[0, block * each + step], ids)
        id_cols_ref[:, block * LANES : (block + 1) * LANES] = ids
    ids = id_cols_ref[...].astype(jnp.float32)
    pixels = ids.shape[1]
    pixel = lax.broadcasted_iota(jnp.int32, ids.shape, 1)
    above = jnp.where(pixel < cols, -1.0, pltpu.roll(ids, cols, 1))
    below = jnp.where(pixel >= pixels - cols, -1.0, pltpu.roll(ids, pixels - cols, 1))
    lanes_ref[0:1, :] = jnp.where(above == ids, 1.0, 0.0)[0:1]
    lanes_ref[1:2, :] = jnp.where(below == ids, 1.0, 0.0)[0:1]


def place_pieces(pieces, whole_ref, sems):
    own_pixels = whole_ref.shape[0] // len(pieces)
    height = lax.axis_index("height")
    copies = []
    for place, piece in enumerate(pieces):
        start = pl.multiple_of((height ^ place) * own_pixels, own_pixels)
        rows = pl.ds(start, own_pixels)
        copies.append(pltpu.make_async_copy(piece, whole_ref.at[rows, :], sems.at[place]))
    return copies


def hold_kernel(
    ids_hbm,
    gains_hbm,
    shifts_hbm,
    biases_hbm,
    weights_hbm,
    qkv_hbm,
    proj_hbm,
    qv_bias_hbm,
    proj_bias_hbm,
    weights_ref,
    turned_ref,
    qkv_ref,
    proj_ref,
    table_ref,
    mask_ref,
    lanes_ref,
    id_rows_ref,
    id_cols_ref,
    ids_ref,
    gains_ref,
    shifts_ref,
    biases_ref,
    qv_bias_ref,
    proj_bias_ref,
    sems,
    *,
    cols,
):
    channels = weights_ref.shape[-1]
    small = [
        (ids_hbm, ids_ref),
        (gains_hbm, gains_ref),
        (shifts_hbm, shifts_ref),
        (biases_hbm, biases_ref),
        (qv_bias_hbm, qv_bias_ref),
        (proj_bias_hbm, proj_bias_ref),
    ]
    large = [(weights_hbm, weights_ref), (qkv_hbm, qkv_ref), (proj_hbm, proj_ref)]
    for which in range(2):
        for row_tap in range(3):
            for col_tap in range(3):
                place = slice(col_tap * channels, (col_tap + 1) * channels)
                large.append(
                    (
                        weights_hbm.at[which, 2 - row_tap, 2 - col_tap],
                        turned_ref.at[which, row_tap, :, place],
                    )
                )
    copies = [
        pltpu.make_async_copy(source, target, sems.at[index])
        for index, (source, target) in enumerate(small + large)
    ]
    for copy in copies:
        copy.start()
    for copy in copies[: len(small)]:
        copy.wait()
    build_masks(ids_ref, mask_ref, lanes_ref, id_rows_ref, id_cols_ref, cols)
    table_ref[6:9, :] = gains_ref[...]
    table_ref[9:12, :] = shifts_ref[...]
    table_ref[12:14, :] = biases_ref[...]
    table_ref[14:16, :] = qv_bias_ref[...]
    table_ref[16:17, :] = proj_bias_ref[...]
    for copy in copies[len(small) :]:
        copy.wait()


def conv_kernel(*refs, cols, count):
    pieces, refs = refs[:count], refs[count:]
    (
        weights_ref,
        params_ref,
        mask_ref,
        features_ref,
        act_one_ref,
        middle_ref,
        act_two_ref,
        residual_ref,
        table_ref,
        own_ref,
        taps_ref,
        sem,
    ) = refs
    pixels, channels = features_ref.shape
    wide = jnp.float32
    own_copy = pltpu.make_async_copy(pieces[0], own_ref, sem)
    own_copy.start()
    table_ref[...] = params_ref[...]
    clear_edges(taps_ref, cols)

    def read_input(rows):
        return features_ref[rows, :].astype(wide)

    def read_middle(rows):
        return middle_ref[rows, :]

    height = lax.axis_index("height")
    own_pixels = pixels // count
    seen = RunningStats()
    for place in list(range(1, count)) + [0]:
        if place == 0:
            own_copy.wait()
        piece = (pieces[place] if place else own_ref)[...]
        start = pl.multiple_of((height ^ place) * own_pixels, own_pixels)
        features_ref[pl.ds(start, own_pixels), :] = piece
        seen.add(piece.astype(wide))
    table_ref[0:1, :], table_ref[1:2, :] = seen.finish(pixels)
    seen = RunningStats()

    def keep(rows, value):
        seen.add(value)
        return value

    run_conv(
        taps_ref,
        product_forward(weights_ref.at[0]),
        mask_ref,
        middle_ref,
        activation(read_input, *norm_rows(table_ref, 0), act_one_ref, taps_ref, cols),
        lambda rows, part: part + table_ref[12:13, :],
        keep,
        cols,
    )
    table_ref[2:3, :], table_ref[3:4, :] = seen.finish(pixels)
    seen = RunningStats()
    run_conv(
        taps_ref,
        product_forward(weights_ref.at[1]),
        mask_ref,
        residual_ref,
        activation(read_middle, *norm_rows(table_ref, 1), act_two_ref, taps_ref, cols),
        lambda rows, part: part + (read_input(rows) + table_ref[13:14, :]),
        keep,
        cols,
    )
    table_ref[4:5, :], table_ref[5:6, :] = seen.finish(pixels)


def score_kernel(
    qkv_ref,
    proj_ref,
    residual_ref,
    table_ref,
    id_rows_ref,
    id_cols_ref,
    normed_ref,
    query_ref,
    key_ref,
    value_ref,
    soft_ref,
    out_flip_ref,
    output_ref,
    value_flip_ref,
    *,
    score_scale,
):
    pixels, channels = residual_ref.shape
    own_pixels = output_ref.shape[0]
    wide = jnp.float32
    exponent = score_scale * 1.4426950408889634
    mean, inverse, gain, shift = norm_rows(table_ref, 2)
    scale = inverse * gain
    block = min(QUERY_ROWS, pixels)

    def project(rows, carry):
        normed = ((residual_ref[rows, :] - mean) * scale + shift).astype(jnp.bfloat16)
        normed_ref[rows, :] = normed
        query_ref[rows, :] = (
            jnp.dot(normed, qkv_ref[:, 0:channels], preferred_element_type=wide)
            + table_ref[14:15, :]
        ).astype(jnp.bfloat16)
        key_ref[rows, :] = jnp.dot(
            normed, qkv_ref[:, channels : 2 * channels], preferred_element_type=wide
        ).astype(jnp.bfloat16)
        values = (
            jnp.dot(normed, qkv_ref[:, 2 * channels :], preferred_element_type=wide)
            + table_ref[15:16, :]
        ).astype(jnp.bfloat16)
        value_ref[rows, :] = values
        value_flip_ref[:, rows] = values.T
        return carry

    each_block(pixels, block, project)

    def attend(rows, carry):
        scores = lax.dot_general(
            key_ref[...], query_ref[rows, :], (((1,), (1,)), ((), ())), preferred_element_type=wide
        )
        same = widen(id_rows_ref[...], block) == id_cols_ref[0:1, rows]
        scores = jnp.where(same, scores, masked_score)
        scores = jnp.exp2((scores - jnp.max(scores, axis=0, keepdims=True)) * exponent)
        weights = scores * (1.0 / jnp.sum(scores, axis=0, keepdims=True))
        soft_ref[:, rows] = weights.astype(jnp.bfloat16)
        return carry

    each_block(pixels, block, attend)

    def collect(rows, carry):
        out_flip_ref[rows, :] = jnp.dot(
            value_flip_ref[rows, :], soft_ref[...], preferred_element_type=wide
        ).astype(jnp.bfloat16)
        return carry

    each_block(channels, channels // 2, collect)
    height = lax.axis_index("height")
    own = pl.ds(pl.multiple_of(height * own_pixels, own_pixels), own_pixels)
    output_ref[...] = (
        residual_ref[own, :]
        + lax.dot_general(
            out_flip_ref[:, own],
            proj_ref[...],
            (((0,), (0,)), ((), ())),
            preferred_element_type=wide,
        )
        + table_ref[16:17, :]
    ).astype(jnp.bfloat16)


def own_quarter():
    height = lax.axis_index("height")
    return (height & 1) * 2 + ((height >> 1) & 1)


def send_order(source_ref, targets, axis, share):
    me = lax.axis_index("canvas")
    for step, target in enumerate(targets):
        place = pl.ds(pl.multiple_of((me ^ step) * share, share), share)
        target[...] = source_ref[place, :] if axis == 0 else source_ref[:, place]


def attention_kernel(
    proj_ref,
    normed_ref,
    query_ref,
    key_ref,
    value_ref,
    soft_ref,
    out_flip_ref,
    *refs,
    score_scale,
    count,
):
    pieces, (grad_ref, packed_ref, sums_ref), refs = (
        refs[:count],
        refs[count : count + 3],
        refs[count + 3 :],
    )
    *mixed_refs, mixed_ref, key_flip_ref, back_ref, score_grad_ref, flip_ref, sems = refs
    pixels, channels = normed_ref.shape
    block = min(QUERY_ROWS, pixels)
    wide = jnp.float32
    copies = place_pieces(pieces, grad_ref, sems)
    for copy in copies:
        copy.start()
    quarter = channels // 4
    own = pl.ds(pl.multiple_of(own_quarter() * quarter, quarter), quarter)
    flip_ref[...] = normed_ref[:, own].T
    key_flip_ref[...] = key_ref[...].T
    for copy in copies:
        copy.wait()

    for start in range(0, pixels, block):
        rows = slice(start, start + block)
        back_ref[rows, :] = lax.dot_general(
            grad_ref[rows, :], proj_ref[...], (((1,), (1,)), ((), ())), preferred_element_type=wide
        ).astype(jnp.bfloat16)
    for start in range(0, pixels, block):
        rows = slice(start, start + block)
        weights = soft_ref[:, rows].astype(wide)
        weight_grad = lax.dot_general(
            value_ref[...],
            back_ref[rows, :],
            (((1,), (1,)), ((), ())),
            preferred_element_type=wide,
        )
        dots = jnp.sum(weights * weight_grad, axis=0, keepdims=True)
        score_grad = (weights * (weight_grad - dots)).astype(jnp.bfloat16)
        score_grad_ref[:, rows] = score_grad
        query_grad = jnp.dot(key_flip_ref[...], score_grad, preferred_element_type=wide)
        packed_ref[rows, 0:channels] = (query_grad * score_scale).astype(jnp.bfloat16).T
        packed_ref[rows, 2 * channels :] = jnp.dot(
            soft_ref[rows, :], back_ref[...], preferred_element_type=wide
        ).astype(jnp.bfloat16)
    for start in range(0, pixels, block):
        rows = slice(start, start + block)
        packed_ref[rows, channels : 2 * channels] = (
            jnp.dot(score_grad_ref[rows, :], query_ref[...], preferred_element_type=wide)
            * score_scale
        ).astype(jnp.bfloat16)

    def pack(rows, carry):
        return (
            carry[0] + fold(packed_ref[rows, 0:channels].astype(wide)),
            carry[1] + fold(packed_ref[rows, 2 * channels :].astype(wide)),
            carry[2] + fold(grad_ref[rows, :].astype(wide)),
        )

    zeros = jnp.zeros((8, channels), wide)
    totals = zeros, zeros, zeros
    for start in range(0, pixels, CHUNK):
        totals = pack(pl.ds(start, CHUNK), totals)
    sums_ref[...] = jnp.zeros(sums_ref.shape, wide)
    for row, total in enumerate(totals):
        sums_ref[8 + row : 9 + row, :] = column_total(total)
    mixed_ref[:, 0 : 3 * channels] = jnp.dot(
        flip_ref[...], packed_ref[...], preferred_element_type=wide
    ).astype(jnp.bfloat16)
    mixed_ref[:, 3 * channels :] = jnp.dot(
        out_flip_ref[own, :], grad_ref[...], preferred_element_type=wide
    ).astype(jnp.bfloat16)
    send_order(mixed_ref, mixed_refs, 0, quarter // len(mixed_refs))


def third_kernel(
    qkv_ref,
    grad_ref,
    packed_ref,
    residual_ref,
    table_ref,
    act_two_ref,
    lanes_ref,
    old_sums_ref,
    residual_grad_ref,
    grad_two_ref,
    sums_ref,
    keep_ref,
    send_ref,
    total_ref,
    flip_ref,
    columns_ref,
    part_ref,
    *,
    cols,
):
    pixels, channels = residual_ref.shape
    block = pixels
    wide = jnp.float32
    mean, inverse, gain, shift = norm_rows(table_ref, 2)
    zeros = jnp.zeros((8, channels), wide)

    sums = (zeros, zeros)
    for start in range(0, pixels, block):
        rows = pl.ds(start, block)
        normed_grad = lax.dot_general(
            packed_ref[rows, :], qkv_ref[...], (((1,), (1,)), ((), ())), preferred_element_type=wide
        )
        total_ref[rows, :] = normed_grad
        normed = (residual_ref[rows, :] - mean) * inverse
        sums = sums[0] + fold(normed_grad), sums[1] + fold(normed_grad * normed)
    sums_ref[...] = old_sums_ref[...]
    sums_ref[5:6, :] = column_total(sums[1])
    sums_ref[6:7, :] = column_total(sums[0])
    mean_grad, mean_cross = back_means(sums, gain, pixels)

    def finish(rows, carry):
        normed = (residual_ref[rows, :] - mean) * inverse
        back = inverse * (total_ref[rows, :] * gain - mean_grad - normed * mean_cross)
        total = grad_ref[rows, :].astype(wide) + back
        residual_grad_ref[rows, :] = total
        low = total.astype(jnp.bfloat16)
        grad_two_ref[rows, :] = low
        return carry + fold(low.astype(wide))

    sums_ref[7:8, :] = column_total(each_chunk(pixels, finish, zeros))
    weight_part(act_two_ref, grad_two_ref, lanes_ref, flip_ref, columns_ref, part_ref, cols)
    keep_half(part_ref, 2, 1, keep_ref, send_ref)


def second_kernel(
    total_ref,
    partial_ref,
    middle_ref,
    table_ref,
    act_one_ref,
    lanes_ref,
    old_sums_ref,
    grad_one_ref,
    sums_ref,
    keep_ref,
    send_ref,
    flip_ref,
    columns_ref,
    part_ref,
    *,
    cols,
):
    pixels, channels = middle_ref.shape
    sums = partial_ref[0:8, :], partial_ref[8:16, :]
    back = norm_back(total_ref, sums, lambda rows: middle_ref[rows, :], table_ref, 1)
    sums_ref[...] = old_sums_ref[...]
    sums_ref[2:3, :] = column_total(sums[1])
    sums_ref[3:4, :] = column_total(sums[0])

    def finish(rows, carry):
        low = back(rows).astype(jnp.bfloat16)
        grad_one_ref[rows, :] = low
        return carry + fold(low.astype(jnp.float32))

    zeros = jnp.zeros((8, channels), jnp.float32)
    sums_ref[4:5, :] = column_total(each_chunk(pixels, finish, zeros))
    weight_part(act_one_ref, grad_one_ref, lanes_ref, flip_ref, columns_ref, part_ref, cols)
    keep_half(part_ref, 1, 2, keep_ref, send_ref)


def keep_half(part_ref, near, far, keep_ref, send_ref):
    me = lax.axis_index("canvas")
    rows, width = part_ref.shape[0], keep_ref.shape[1]
    for target_ref, flip in ((keep_ref, 0), (send_ref, near)):
        for slot in range(2):
            owner = me ^ flip ^ (slot * far)
            place = pl.ds(pl.multiple_of(owner * width, width), width)
            target_ref[slot * rows : (slot + 1) * rows, :] = part_ref[:, place]


def begin_kernel(grad_ref, mask_ref, weights_ref, total_ref, taps_ref, *, cols):
    begin_back(grad_ref, weights_ref.at[0], mask_ref, taps_ref, total_ref, cols)


def first_kernel(
    old_total_ref,
    taps_ref,
    features_ref,
    table_ref,
    mask_ref,
    old_sums_ref,
    weights_ref,
    own_ref,
    sums_ref,
    partial_ref,
    total_ref,
    *,
    cols,
):
    def read(rows):
        return features_ref[rows, :].astype(jnp.float32)

    sums = finish_back(
        weights_ref.at[0],
        mask_ref,
        taps_ref,
        total_ref,
        read,
        table_ref,
        0,
        cols,
        old_total_ref,
    )
    partial_ref[0:8, :], partial_ref[8:16, :] = sums
    sums_ref[...] = old_sums_ref[...]
    sums_ref[0:1, :] = column_total(sums[1])
    sums_ref[1:2, :] = column_total(sums[0])
    count = own_ref.shape[0]
    own = pl.ds(pl.multiple_of(lax.axis_index("height") * count, count), count)
    own_ref[...] = total_ref[own, :]


def own_kernel(
    own_ref,
    partial_ref,
    features_ref,
    residual_grad_ref,
    table_ref,
    packed_ref,
    old_qkv,
    old_proj,
    input_grad_ref,
    qkv_hbm,
    proj_hbm,
    qkv_ref,
    proj_ref,
    sems,
):
    copies = spread_quarters([packed_ref], [2], qkv_ref, proj_ref, qkv_hbm, proj_hbm, sems)
    mean, inverse, gain, shift = norm_rows(table_ref, 0)
    pixels = features_ref.shape[0]
    sums = partial_ref[0:8, :], partial_ref[8:16, :]
    mean_grad, mean_cross = back_means(sums, gain, pixels)
    count = own_ref.shape[0]
    own = pl.ds(pl.multiple_of(lax.axis_index("height") * count, count), count)
    normed = (features_ref[own, :].astype(jnp.float32) - mean) * inverse
    back = inverse * (own_ref[...] * gain - mean_grad - normed * mean_cross)
    input_grad_ref[...] = (residual_grad_ref[own, :] + back).astype(jnp.bfloat16)
    for copy in copies:
        copy.wait()


def place_kernel(*refs):
    joints, (qkv_hbm, proj_hbm, packed_ref, qkv_ref, proj_ref, sems) = refs[:-6], refs[-6:]
    share = packed_ref.shape[0] // len(joints)
    me = lax.axis_index("canvas")
    for step, joint in enumerate(joints):
        place = pl.ds(pl.multiple_of((me ^ step) * share, share), share)
        packed_ref[place, :] = joint[...]
    copies = spread_quarters([packed_ref], [0], qkv_ref, proj_ref, qkv_hbm, proj_hbm, sems)
    for copy in copies:
        copy.wait()


def spread_quarters(packed, flips, qkv_ref, proj_ref, qkv_hbm, proj_hbm, sems):
    quarter = packed[0].shape[0]
    inner = qkv_ref.shape[2]
    copies = []
    for index, packed_ref in enumerate(packed):
        owner = own_quarter() ^ flips[index]
        rows = pl.ds(pl.multiple_of(owner * quarter, quarter), quarter)
        qkv_ref[index] = packed_ref[:, 0:inner].astype(jnp.float32)
        proj_ref[index] = packed_ref[:, inner:].astype(jnp.float32)
        for which, (held, target) in enumerate(((qkv_ref, qkv_hbm), (proj_ref, proj_hbm))):
            copy = pltpu.make_async_copy(held.at[index], target.at[rows, :], sems.at[index, which])
            copy.start()
            copies.append(copy)
    return copies


def join_kernel(
    old_qkv, old_proj, chip_ref, both_ref, qkv_hbm, proj_hbm, qkv_ref, proj_ref, sems
):
    copies = spread_quarters(
        [chip_ref, both_ref], [1, 3], qkv_ref, proj_ref, qkv_hbm, proj_hbm, sems
    )
    for copy in copies:
        copy.wait()


def halve_kernel(keep_ref, got_ref, hold_ref, send_ref):
    total = keep_ref[...].astype(jnp.float32) + got_ref[...].astype(jnp.float32)
    rows = hold_ref.shape[0]
    hold_ref[...] = total[0:rows]
    send_ref[...] = total[rows:].astype(jnp.bfloat16)


def sums_kernel(
    sums_ref,
    got_sums_ref,
    hold_one_ref,
    got_one_ref,
    hold_two_ref,
    got_two_ref,
    share_ref,
    gains_ref,
    shifts_ref,
    conv_ref,
    qv_ref,
    proj_ref,
):
    for which, (hold_ref, got_ref) in enumerate(
        ((hold_one_ref, got_one_ref), (hold_two_ref, got_two_ref))
    ):
        total = hold_ref[...] + got_ref[...].astype(jnp.float32)
        share_ref[which] = total.reshape(share_ref.shape[1:])
    total = sums_ref[...] + got_sums_ref[...]
    for row, start in enumerate((0, 2, 5)):
        gains_ref[row : row + 1, :] = total[start : start + 1]
        shifts_ref[row : row + 1, :] = total[start + 1 : start + 2]
    conv_ref[0:1, :] = total[4:5]
    conv_ref[1:2, :] = total[7:8]
    qv_ref[...] = total[8:10]
    proj_ref[...] = total[10:11]


def call_kernel(kernel, outputs, scratch, operands, places, flops, limit, out_places=None, aliases={}):
    out_places = out_places or "v" * len(outputs)
    spaces = {
        "v": pl.BlockSpec(memory_space=pltpu.VMEM),
        "s": pl.BlockSpec(memory_space=pltpu.SMEM),
        "h": pl.BlockSpec(memory_space=pl.ANY),
        "o": pl.BlockSpec(memory_space=pltpu.VMEM),
        "a": pl.BlockSpec(memory_space=pl.ANY),
    }
    moved = 8 * flops // LANES
    held = {"v": pltpu.VMEM, "h": pltpu.HBM, "o": jax.ShapeDtypeStruct}
    operands = [
        pltpu.with_memory_space_constraint(array, pltpu.HBM) if place == "h" else array
        for array, place in zip(operands, places)
    ]
    return pl.pallas_call(
        kernel,
        out_shape=[held[place](*output) for output, place in zip(outputs, out_places)],
        in_specs=[spaces[place] for place in places],
        out_specs=[spaces[place] for place in out_places],
        scratch_shapes=scratch,
        input_output_aliases=aliases,
        compiler_params=pltpu.CompilerParams(vmem_limit_bytes=limit * 2**20),
        cost_estimate=pl.CostEstimate(flops=flops, bytes_accessed=moved, transcendentals=0),
    )(*operands)


def send_height(block, step):
    size = lax.axis_size("height")
    return lax.ppermute(block, "height", [(i, i ^ step) for i in range(size)])


def with_cores(blocks):
    return [piece for block in blocks for piece in (block, send_height(block, 1))]


def send_canvas(block, step):
    size = lax.axis_size("canvas")
    return lax.ppermute(block, "canvas", [(i, i ^ step) for i in range(size)])


def trade_canvas(pieces):
    return [pieces[0]] + [send_canvas(piece, step) for step, piece in enumerate(pieces) if step]


def whole_canvas(
    features,
    tile_ids,
    norm_gains,
    norm_shifts,
    conv_weights,
    conv_biases,
    qkv_weight,
    qv_bias,
    proj_weight,
    proj_bias,
    cotangent,
):
    height_size = lax.axis_size("height")
    canvas_size = lax.axis_size("canvas")
    local_rows, cols, channels = features.shape[1:]
    all_rows = tile_ids.shape[1]
    pixels = all_rows * cols
    own_pixels = local_rows * cols
    out_share = channels // height_size
    ci_share = channels // canvas_size
    quarter = channels // 4
    row_share = quarter // canvas_size
    low, wide = jnp.bfloat16, jnp.float32

    own_features = features.reshape(own_pixels, channels)
    own_grad = cotangent.reshape(own_pixels, channels)
    steps = range(2, height_size, 2)
    held_features = [own_features] + [send_height(own_features, step) for step in steps]
    plane = ((pixels, channels), low)
    plane_wide = ((pixels, channels), wide)
    sums_shape = ((16, channels), wide)
    mixed_shapes = [((row_share, 4 * channels), low)] * canvas_size
    taps = pltpu.VMEM((pixels + 2 * cols, 3 * channels), low)
    held_wide = pltpu.VMEM((pixels, channels), wide)
    flipped = pltpu.VMEM((channels, pixels), low)
    narrow = pltpu.VMEM((NARROW, pixels), low)
    columns = pltpu.VMEM((9 * out_share, pixels), low)
    part_held = pltpu.VMEM((9 * out_share, channels), low)
    sem = pltpu.SemaphoreType.DMA
    conv_flops = 2 * 9 * pixels * channels * channels
    dot_flops = 2 * pixels * channels * channels
    score_flops = 2 * pixels * pixels * channels
    scale = channels ** (-0.5)

    (
        held_conv,
        turned,
        held_qkv,
        held_proj,
        params,
        mask,
        lane_mask,
        id_rows,
        id_cols,
    ) = call_kernel(
        functools.partial(hold_kernel, cols=cols),
        [
            (conv_weights.shape, low),
            ((2, 3, channels, 3 * channels), low),
            (qkv_weight.shape, low),
            (proj_weight.shape, low),
            ((24, channels), wide),
            ((2, pixels, LANES), wide),
            ((8, pixels), wide),
            ((pixels, LANES), jnp.int32),
            ((8, pixels), jnp.int32),
        ],
        [
            pltpu.SMEM(tile_ids.shape, jnp.int32),
            pltpu.VMEM(norm_gains.shape, wide),
            pltpu.VMEM(norm_shifts.shape, wide),
            pltpu.VMEM(conv_biases.shape, wide),
            pltpu.VMEM(qv_bias.shape, wide),
            pltpu.VMEM((1, channels), wide),
            sem((27,)),
        ],
        [
            tile_ids,
            norm_gains,
            norm_shifts,
            conv_biases,
            conv_weights,
            qkv_weight,
            proj_weight,
            qv_bias,
            proj_bias.reshape(1, channels),
        ],
        "h" * 9,
        conv_flops,
        8,
    )
    held_features[1:] = [
        lax.optimization_barrier((params, block))[1] for block in held_features[1:]
    ]
    pieces = with_cores(held_features)
    far_grad, *pieces[4::2] = lax.optimization_barrier((own_grad, *held_features[2:]))
    held_grads = [own_grad, send_height(own_grad, 2)]
    held_grads[1], pieces[2] = lax.optimization_barrier((held_grads[1], held_features[1]))
    held_grads += [send_height(far_grad, step) for step in steps[1:]]

    all_features, act_one, middle, act_two, residual, table = call_kernel(
        functools.partial(conv_kernel, cols=cols, count=height_size),
        [plane, plane, plane_wide, plane, plane_wide, ((24, channels), wide)],
        [pltpu.VMEM((own_pixels, channels), low), taps, sem],
        [*pieces, held_conv, params, mask],
        "h" + "v" * (height_size + 2),
        2 * conv_flops,
        16,
    )
    residual, *held_grads = lax.optimization_barrier((residual, *held_grads))
    grad_pieces = with_cores(held_grads)
    normed, query, key, value, soft, out_flip, output = call_kernel(
        functools.partial(score_kernel, score_scale=scale),
        [
            plane,
            plane,
            plane,
            plane,
            ((pixels, pixels), low),
            ((channels, pixels), low),
            ((own_pixels, channels), low),
        ],
        [
            flipped,
        ],
        [
            held_qkv,
            held_proj,
            residual,
            table,
            id_rows,
            id_cols,
        ],
        "vvvvvv",
        3 * dot_flops + 2 * score_flops,
        16,
        "v" * 6 + "o",
    )
    normed, *grad_pieces = lax.optimization_barrier((normed, *grad_pieces))
    all_grad, packed, sums, *mixed = call_kernel(
        functools.partial(attention_kernel, score_scale=scale, count=height_size),
        [plane, ((pixels, 3 * channels), low), sums_shape, *mixed_shapes],
        [
            pltpu.VMEM((quarter, 4 * channels), low),
            flipped,
            pltpu.VMEM((pixels, channels), low),
            pltpu.VMEM((pixels, pixels), low),
            pltpu.VMEM((quarter, pixels), low),
            sem((height_size,)),
        ],
        [held_proj, normed, query, key, value, soft, out_flip, *grad_pieces],
        "vvvvvvvh" + "a" * (height_size - 1),
        3 * dot_flops + 4 * score_flops,
        20,
    )
    mixed = trade_canvas(mixed)
    halves = [((18 * out_share, ci_share), low)] * 2
    residual_grad, grad_two, sums, keep_two, send_two = call_kernel(
        functools.partial(third_kernel, cols=cols),
        [plane_wide, plane, sums_shape, *halves],
        [held_wide, narrow, columns, part_held],
        [held_qkv, all_grad, packed, residual, table, act_two, lane_mask, sums],
        "vvvvvvvv",
        3 * dot_flops + conv_flops // height_size,
        16,
    )
    grad_two, *mixed = lax.optimization_barrier((grad_two, *mixed))
    mixed_sum = mixed[0].astype(wide)
    for piece in mixed[1:]:
        mixed_sum = mixed_sum + piece.astype(wide)
    joints = trade_canvas([mixed_sum.astype(low)] * canvas_size)
    act_two_grad, partial_sums = call_kernel(
        functools.partial(turn_kernel, cols=cols),
        [plane_wide, sums_shape],
        [taps],
        [grad_two, mask, turned, middle, table],
        "vvvvv",
        conv_flops,
        16,
    )
    act_two_grad, *joints = lax.optimization_barrier((act_two_grad, *joints))
    qkv_grad, proj_grad, own_mixed = call_kernel(
        place_kernel,
        [(qkv_weight.shape, wide), (proj_weight.shape, wide), ((quarter, 4 * channels), low)],
        [
            pltpu.VMEM((1, quarter, 3 * channels), wide),
            pltpu.VMEM((1, quarter, channels), wide),
            sem((1, 2)),
        ],
        joints,
        "v" * canvas_size,
        0,
        12,
        "hhv",
    )
    own_mixed, send_two = lax.optimization_barrier((own_mixed, send_two))
    got_two = send_canvas(send_two, 2)
    chip_mixed = send_height(own_mixed, 2)
    core_mixed = send_height(own_mixed, 1)
    grad_one, sums, keep_one, send_one = call_kernel(
        functools.partial(second_kernel, cols=cols),
        [plane, sums_shape, *halves],
        [narrow, columns, part_held],
        [act_two_grad, partial_sums, middle, table, act_one, lane_mask, sums],
        "vvvvvvv",
        1,
        16,
    )
    got_one = send_canvas(send_one, 1)

    def halve(keep, got):
        return call_kernel(
            halve_kernel,
            [((9 * out_share, ci_share), kind) for kind in (wide, low)],
            [],
            [keep, got],
            "vv",
            0,
            12,
        )

    half_total, half_taps = call_kernel(
        functools.partial(begin_kernel, cols=cols),
        [plane_wide, (taps.shape, low)],
        [],
        [grad_one, mask, turned],
        "vvv",
        1,
        16,
    )
    half_total, got_two = lax.optimization_barrier((half_total, got_two))
    hold_two, send_two = halve(keep_two, got_two)
    got_two = send_canvas(send_two, 1)
    half_total, hold_two = lax.optimization_barrier((half_total, hold_two))
    own_total, sums, partial_sums = call_kernel(
        functools.partial(first_kernel, cols=cols),
        [((own_pixels, channels), wide), sums_shape, sums_shape],
        [held_wide],
        [half_total, half_taps, all_features, table, mask, sums, turned],
        "vvvvvvv",
        conv_flops // 3,
        16,
    )
    sums, core_mixed, got_one = lax.optimization_barrier((sums, core_mixed, got_one))
    got_sums = send_canvas(sums, 1)
    hold_one, send_one = halve(keep_one, got_one)
    got_one = send_canvas(send_one, 2)
    own_total, hold_one = lax.optimization_barrier((own_total, hold_one))
    quarter_scratch = [
        pltpu.VMEM((2, quarter, 3 * channels), wide),
        pltpu.VMEM((2, quarter, channels), wide),
        sem((2, 2)),
    ]
    grad_shapes = [(qkv_weight.shape, wide), (proj_weight.shape, wide)]
    input_grad, qkv_grad, proj_grad = call_kernel(
        own_kernel,
        [((own_pixels, channels), low), *grad_shapes],
        quarter_scratch,
        [
            own_total,
            partial_sums,
            all_features,
            residual_grad,
            table,
            core_mixed,
            qkv_grad,
            proj_grad,
        ],
        "vvvvvvhh",
        conv_flops,
        12,
        "ohh",
        {6: 1, 7: 2},
    )
    input_grad, got_sums, chip_mixed, got_one, got_two = lax.optimization_barrier(
        (input_grad, got_sums, chip_mixed, got_one, got_two)
    )
    both_mixed = send_height(chip_mixed, 1)
    sums = sums + got_sums
    got_sums = send_canvas(sums, 2)
    qkv_grad, proj_grad = call_kernel(
        join_kernel,
        grad_shapes,
        quarter_scratch,
        [qkv_grad, proj_grad, chip_mixed, both_mixed],
        "hhvv",
        0,
        12,
        "hh",
        {0: 0, 1: 1},
    )
    qkv_grad, got_sums = lax.optimization_barrier((qkv_grad, got_sums))
    vector_shapes = [norm_gains.shape, norm_shifts.shape, conv_biases.shape, qv_bias.shape]
    conv_grad, gains_grad, shifts_grad, biases_grad, qv_grad, proj_bias_grad = call_kernel(
        sums_kernel,
        [((2, 3, 3, out_share, ci_share), wide)]
        + [(shape, wide) for shape in vector_shapes + [(1, channels)]],
        [],
        [sums, got_sums, hold_one, got_one, hold_two, got_two],
        "vvvvvv",
        0,
        12,
        "o" * 6,
    )
    own_shape = (1, local_rows, cols, channels)
    return (
        output.reshape(own_shape),
        input_grad.reshape(own_shape),
        gains_grad,
        shifts_grad,
        jnp.swapaxes(conv_grad, 3, 4),
        biases_grad,
        qkv_grad,
        qv_grad,
        proj_grad,
        proj_bias_grad.reshape(channels),
    )


def on_device(*arrays):
    features, tile_ids = arrays[0], arrays[1]
    local_rows, cols, channels = features.shape[1:]
    pixels = tile_ids.shape[1] * cols
    height_size, canvas_size = lax.axis_size("height"), lax.axis_size("canvas")
    powers = all(size & (size - 1) == 0 for size in (height_size, canvas_size, cols))
    fits = (
        powers
        and height_size > 2
        and canvas_size == 4
        and channels == LANES * canvas_size
        and pixels <= MOST_PIXELS
        and pixels % FILL_ROWS == 0
        and FILL_ROWS % CHUNK == 0
        and pixels % KEY_ROWS == 0
        and (local_rows * cols) % LANES == 0
        and CHUNK % cols == 0
        and cols % 16 == 0
        and channels % (LANES * canvas_size) == 0
        and 2 * channels == NARROW * height_size
    )
    return whole_canvas(*arrays) if fits else split_canvas(*arrays)


def solution(mesh):
    in_specs = (
        P("canvas", "height", None, None),
        P("canvas", None),
        P(),
        P(),
        P(),
        P(),
        P(),
        P(),
        P(),
        P(),
        P("canvas", "height", None, None),
    )
    out_specs = (
        P("canvas", "height", None, None),
        P("canvas", "height", None, None),
        P(),
        P(),
        P(None, None, None, "canvas", "height"),
        P(),
        P(),
        P(),
        P(),
        P(),
    )
    return jax.shard_map(
        on_device, mesh=mesh, in_specs=in_specs, out_specs=out_specs, check_vma=False
    )
```

```python
import functools

import jax
import jax.numpy as jnp
from jax import lax
from jax.experimental import pallas as pl
from jax.experimental.pallas import tpu as pltpu
from jax.sharding import PartitionSpec as P

GROUPS = 32


epsilon = 1e-06
masked_score = -1e30
MOST_PIXELS = 1024
LANES = 128
NARROW = 128
CHUNK = 128
FILL_ROWS = 256
QUERY_ROWS = 512


def extended(block, sides, width):
    for axis, dim in sides:
        count = lax.axis_size(axis)
        forward = [(i, i + 1) for i in range(count - 1)]
        backward = [(target, source) for source, target in forward]
        low = lax.ppermute(
            lax.slice_in_dim(block, block.shape[dim] - width, None, axis=dim), axis, forward
        )
        high = lax.ppermute(lax.slice_in_dim(block, 0, width, axis=dim), axis, backward)
        block = jnp.concatenate([low, block, high], axis=dim)
    return block


def group_total(vector):
    return vector.reshape(GROUPS, -1).sum(axis=1)


def spread_groups(vector, channels):
    return jnp.repeat(vector, channels // GROUPS)


def norm_forward(values, gain, shift, members):
    channels = values.shape[1]
    totals = lax.psum(group_total(jnp.sum(values, axis=0)), "height")
    centered = values - spread_groups(totals / members, channels)
    squares = lax.psum(group_total(jnp.sum(centered * centered, axis=0)), "height")
    inverse = spread_groups(lax.rsqrt(squares / members + epsilon), channels)
    normed = centered * inverse
    return (normed, inverse, normed * gain + shift)


def norm_backward(grad_in, normed, inverse, gain, members):
    channels = grad_in.shape[1]
    scaled = grad_in * gain
    both_sums = lax.psum(
        (group_total(jnp.sum(scaled, axis=0)), group_total(jnp.sum(scaled * normed, axis=0))),
        "height",
    )
    mean_grad = spread_groups(both_sums[0] / members, channels)
    mean_cross = spread_groups(both_sums[1] / members, channels)
    result = inverse * (scaled - mean_grad - normed * mean_cross)
    return (result, jnp.sum(grad_in * normed, axis=0), jnp.sum(grad_in, axis=0))


def swish(values):
    return values * jax.nn.sigmoid(values)


def swish_slope(values):
    sigmoid_part = jax.nn.sigmoid(values)
    return sigmoid_part * (1.0 + values * (1.0 - sigmoid_part))


def tap_columns(padded, row_mask, local_rows, canvas_cols):
    pieces = []
    for row_tap in range(3):
        rows_taken = padded[row_tap : row_tap + local_rows] * row_mask[:, row_tap, None, None]
        for col_tap in range(3):
            pieces.append(rows_taken[:, col_tap : col_tap + canvas_cols])
    stacked = jnp.concatenate(pieces, axis=2)
    return stacked.reshape(local_rows * canvas_cols, stacked.shape[2])


def conv_forward(acts, row_mask, weight, bias):
    local_rows, canvas_cols, channels = acts.shape
    rimmed = extended(acts, (("height", 0),), 1)
    padded = jnp.pad(rimmed, ((0, 0), (1, 1), (0, 0)))
    gathered = tap_columns(padded, row_mask, local_rows, canvas_cols)
    result = (
        jnp.dot(
            gathered, weight.reshape(9 * channels, channels), preferred_element_type=jnp.float32
        )
        + bias
    )
    return (result, gathered)


def conv_backward(grad_low, row_mask, weight, gathered):
    local_rows, canvas_cols, channels = grad_low.shape
    flat_grad = grad_low.reshape(local_rows * canvas_cols, channels)
    weight_grad = lax.dot_general(
        gathered, flat_grad, (((0,), (0,)), ((), ())), preferred_element_type=jnp.float32
    )
    rimmed = extended(grad_low, (("height", 0),), 1)
    padded = jnp.pad(rimmed, ((0, 0), (1, 1), (0, 0)))
    grad_taps = tap_columns(padded, row_mask, local_rows, canvas_cols)
    flipped = jnp.transpose(weight[::-1, ::-1], (0, 1, 3, 2)).reshape(9 * channels, channels)
    input_part = jnp.dot(grad_taps, flipped, preferred_element_type=jnp.float32)
    return (
        input_part,
        weight_grad.reshape(3, 3, channels, channels),
        jnp.sum(flat_grad.astype(jnp.float32), axis=0),
    )


def take_rows(array, offset, count):
    return lax.dynamic_slice_in_dim(array, offset, count)


def score_grads(
    queries, out_grad, log_total, row_dots, query_ids, key_rows, value_rows, key_ids, score_scale
):
    scores = (
        lax.dot_general(
            queries, key_rows, (((1,), (1,)), ((), ())), preferred_element_type=jnp.float32
        )
        * score_scale
    )
    same_tile = query_ids[:, None] == key_ids[None, :]
    softmax_block = jnp.exp(jnp.where(same_tile, scores - log_total[:, None], masked_score))
    weight_grad = lax.dot_general(
        out_grad, value_rows, (((1,), (1,)), ((), ())), preferred_element_type=jnp.float32
    )
    score_grad = (softmax_block * (weight_grad - row_dots[:, None])).astype(jnp.bfloat16)
    return (softmax_block.astype(jnp.bfloat16), score_grad)


def split_canvas(
    features,
    tile_ids,
    norm_gains,
    norm_shifts,
    conv_weights,
    conv_biases,
    qkv_weight,
    qv_bias,
    proj_weight,
    proj_bias,
    cotangent,
):
    height_size = lax.axis_size("height")
    local_rows = features.shape[1]
    canvas_cols = features.shape[2]
    channels = features.shape[3]
    pixels = local_rows * canvas_cols
    row_ids = tile_ids[0]
    all_rows = row_ids.shape[0]
    members = float(all_rows * canvas_cols * (channels // GROUPS))
    score_scale = channels ** (-0.5)
    first_row = lax.axis_index("height") * local_rows
    edge_ids = jnp.full((1,), -1, jnp.int32)
    padded_ids = jnp.concatenate([edge_ids, row_ids, edge_ids])
    near_ids = lax.dynamic_slice_in_dim(padded_ids, first_row, local_rows + 2)
    own_rows = near_ids[1 : local_rows + 1]
    row_mask = jnp.stack(
        [near_ids[row_tap : row_tap + local_rows] == own_rows for row_tap in range(3)], axis=1
    ).astype(jnp.bfloat16)
    key_ids = jnp.repeat(row_ids, canvas_cols)
    query_ids = jnp.repeat(own_rows, canvas_cols)
    grid_shape = (local_rows, canvas_cols, channels)
    inputs = features[0].reshape(pixels, channels).astype(jnp.float32)
    normed_one, inverse_one, pre_one = norm_forward(inputs, norm_gains[0], norm_shifts[0], members)
    act_one = swish(pre_one).astype(jnp.bfloat16).reshape(grid_shape)
    middle, taps_one = conv_forward(act_one, row_mask, conv_weights[0], conv_biases[0])
    normed_two, inverse_two, pre_two = norm_forward(middle, norm_gains[1], norm_shifts[1], members)
    act_two = swish(pre_two).astype(jnp.bfloat16).reshape(grid_shape)
    branch, taps_two = conv_forward(act_two, row_mask, conv_weights[1], conv_biases[1])
    residual = inputs + branch
    normed_three, inverse_three, pre_three = norm_forward(
        residual, norm_gains[2], norm_shifts[2], members
    )
    attn_input = pre_three.astype(jnp.bfloat16)
    mixed = jnp.dot(attn_input, qkv_weight, preferred_element_type=jnp.float32)
    queries = (mixed[:, :channels] + qv_bias[0]).astype(jnp.bfloat16)
    key_rows = mixed[:, channels : 2 * channels].astype(jnp.bfloat16)
    value_rows = (mixed[:, 2 * channels :] + qv_bias[1]).astype(jnp.bfloat16)
    running_max = jnp.full((pixels,), masked_score, jnp.float32)
    key_piece = lax.all_gather(key_rows, "height", axis=0, tiled=True)
    value_piece = lax.all_gather(value_rows, "height", axis=0, tiled=True)
    scores = (
        lax.dot_general(
            queries, key_piece, (((1,), (1,)), ((), ())), preferred_element_type=jnp.float32
        )
        * score_scale
    )
    same_tile = query_ids[:, None] == key_ids[None, :]
    scores = jnp.where(same_tile, scores, masked_score)
    new_max = jnp.maximum(running_max, jnp.max(scores, axis=1))
    weights = jnp.where(same_tile, jnp.exp(scores - new_max[:, None]), 0.0)
    summed_out = jnp.dot(
        weights.astype(jnp.bfloat16), value_piece, preferred_element_type=jnp.float32
    )
    total_weight = jnp.sum(weights, axis=1)
    log_total = new_max + jnp.log(total_weight)
    attended = summed_out / total_weight[:, None]
    attended_low = attended.astype(jnp.bfloat16)
    output = (
        residual
        + jnp.dot(attended_low, proj_weight, preferred_element_type=jnp.float32)
        + proj_bias
    )
    out_grad = cotangent[0].reshape(pixels, channels)
    out_grad_full = out_grad.astype(jnp.float32)
    proj_grad = lax.dot_general(
        attended_low, out_grad, (((0,), (0,)), ((), ())), preferred_element_type=jnp.float32
    )
    proj_bias_grad = jnp.sum(out_grad_full, axis=0)
    attended_grad = lax.dot_general(
        out_grad, proj_weight, (((1,), (1,)), ((), ())), preferred_element_type=jnp.float32
    ).astype(jnp.bfloat16)
    row_dots = jnp.sum(attended_grad.astype(jnp.float32) * attended, axis=1)
    block_rows = pixels * min(height_size, 8)
    zero_block = jnp.zeros((pixels, channels), jnp.float32)
    key_all, value_all = (
        lax.all_gather(key_rows, "height", axis=0, tiled=True),
        lax.all_gather(value_rows, "height", axis=0, tiled=True),
    )
    query_all, grad_all = (
        lax.all_gather(queries, "height", axis=0, tiled=True),
        lax.all_gather(attended_grad, "height", axis=0, tiled=True),
    )
    total_all, dots_all = (
        lax.all_gather(log_total, "height", axis=0, tiled=True),
        lax.all_gather(row_dots, "height", axis=0, tiled=True),
    )

    def own_query_step(running, block_index):
        offset = block_index * block_rows
        key_part = take_rows(key_all, offset, block_rows)
        rounded, score_grad = score_grads(
            queries,
            attended_grad,
            log_total,
            row_dots,
            query_ids,
            key_part,
            take_rows(value_all, offset, block_rows),
            take_rows(key_ids, offset, block_rows),
            score_scale,
        )
        return (
            running
            + jnp.dot(score_grad, key_part, preferred_element_type=jnp.float32) * score_scale,
            None,
        )

    def own_key_step(running, block_index):
        offset = block_index * block_rows
        query_part = take_rows(query_all, offset, block_rows)
        grad_part = take_rows(grad_all, offset, block_rows)
        rounded, score_grad = score_grads(
            query_part,
            grad_part,
            take_rows(total_all, offset, block_rows),
            take_rows(dots_all, offset, block_rows),
            take_rows(key_ids, offset, block_rows),
            key_rows,
            value_rows,
            query_ids,
            score_scale,
        )
        key_part = (
            lax.dot_general(
                score_grad, query_part, (((0,), (0,)), ((), ())), preferred_element_type=jnp.float32
            )
            * score_scale
        )
        value_part = lax.dot_general(
            rounded, grad_part, (((0,), (0,)), ((), ())), preferred_element_type=jnp.float32
        )
        return ((running[0] + key_part, running[1] + value_part), None)

    block_count = key_all.shape[0] // block_rows
    query_grad, unused_one = lax.scan(own_query_step, zero_block, jnp.arange(block_count))
    (key_grad, value_grad), unused_two = lax.scan(
        own_key_step, (zero_block, zero_block), jnp.arange(block_count)
    )
    query_low = query_grad.astype(jnp.bfloat16)
    key_low = key_grad.astype(jnp.bfloat16)
    value_low = value_grad.astype(jnp.bfloat16)
    stacked_grad = jnp.concatenate([query_low, key_low, value_low], axis=1)
    qkv_grad = lax.dot_general(
        attn_input, stacked_grad, (((0,), (0,)), ((), ())), preferred_element_type=jnp.float32
    )
    qv_grad = jnp.stack(
        [
            jnp.sum(query_low.astype(jnp.float32), axis=0),
            jnp.sum(value_low.astype(jnp.float32), axis=0),
        ]
    )
    normed_grad = lax.dot_general(
        stacked_grad, qkv_weight, (((1,), (1,)), ((), ())), preferred_element_type=jnp.float32
    )
    back_three, gain_three, shift_three = norm_backward(
        normed_grad, normed_three, inverse_three, norm_gains[2], members
    )
    residual_grad = out_grad_full + back_three
    grad_two = residual_grad.astype(jnp.bfloat16).reshape(grid_shape)
    act_two_grad, weight_two_grad, bias_two_grad = conv_backward(
        grad_two, row_mask, conv_weights[1], taps_two
    )
    middle_grad, gain_two, shift_two = norm_backward(
        act_two_grad * swish_slope(pre_two), normed_two, inverse_two, norm_gains[1], members
    )
    grad_one = middle_grad.astype(jnp.bfloat16).reshape(grid_shape)
    act_one_grad, weight_one_grad, bias_one_grad = conv_backward(
        grad_one, row_mask, conv_weights[0], taps_one
    )
    input_back, gain_one, shift_one = norm_backward(
        act_one_grad * swish_slope(pre_one), normed_one, inverse_one, norm_gains[0], members
    )
    input_grad = residual_grad + input_back
    conv_grad = jnp.stack([weight_one_grad, weight_two_grad])
    conv_part = lax.psum_scatter(conv_grad, "height", scatter_dimension=4, tiled=True)
    conv_part = lax.psum_scatter(
        conv_part.astype(jnp.bfloat16), "canvas", scatter_dimension=3, tiled=True
    ).astype(jnp.float32)
    summed = lax.psum(
        (
            jnp.stack([gain_one, gain_two, gain_three]),
            jnp.stack([shift_one, shift_two, shift_three]),
            jnp.stack([bias_one_grad, bias_two_grad]),
            qkv_grad,
            qv_grad,
            proj_grad,
            proj_bias_grad,
        ),
        ("canvas", "height"),
    )
    return (
        output.astype(jnp.bfloat16).reshape((1,) + grid_shape),
        input_grad.astype(jnp.bfloat16).reshape((1,) + grid_shape),
        summed[0],
        summed[1],
        conv_part,
        summed[2],
        summed[3],
        summed[4],
        summed[5],
        summed[6],
    )


def fold(block):
    rows, width = block.shape
    return jnp.sum(block.reshape(rows // 8, 8, width), axis=0)


def group_lanes(block, group):
    lane = lax.broadcasted_iota(jnp.int32, block.shape, 1)
    width = block.shape[1]
    step = 1
    while step < group:
        above = pltpu.roll(block, step, 1)
        below = pltpu.roll(block, width - step, 1)
        block = block + jnp.where((lane & step) != 0, above, below)
        step *= 2
    return block


def group_mean(partial, members):
    spread = group_lanes(partial, partial.shape[1] // GROUPS)
    return jnp.sum(spread, axis=0, keepdims=True) * (1.0 / members)


def widen(block, width):
    return jnp.concatenate([block] * (width // block.shape[1]), axis=1)


def each_block(pixels, block, body, carry=0):
    def step(index, carry):
        return body(pl.ds(pl.multiple_of(index * block, block), block), carry)

    return lax.fori_loop(0, pixels // block, step, carry)


def each_chunk(pixels, body, carry):
    return each_block(pixels, CHUNK, body, carry)


def aligned(start, step):
    return start if isinstance(start, int) else pl.multiple_of(start, step)


class RunningStats:
    def __init__(self, channels):
        self.width = channels // GROUPS
        self.reference = None
        self.sums = self.squares = jnp.zeros((8, channels), jnp.float32)

    def add(self, block):
        if self.reference is None:
            self.reference = group_mean(block[0:8], 8.0 * self.width)
        offset = block - self.reference
        self.sums = self.sums + fold(offset)
        self.squares = self.squares + fold(offset * offset)

    def finish(self, pixels):
        both = group_lanes(jnp.concatenate([self.sums, self.squares], axis=0), self.width)
        share = 1.0 / (pixels * self.width)
        offset = column_total(both[0:8]) * share
        variance = column_total(both[8:16]) * share - offset * offset
        return self.reference + offset, lax.rsqrt(jnp.maximum(variance, 0.0) + epsilon)


def put_taps(taps_ref, block, rows, cols):
    count, channels = block.shape
    place = lax.broadcasted_iota(jnp.int32, block.shape, 0) & (cols - 1)
    left = jnp.where(place == 0, 0.0, pltpu.roll(block, 1, 0))
    right = jnp.where(place == cols - 1, 0.0, pltpu.roll(block, count - 1, 0))
    inner = pl.ds(aligned(rows.start + cols, cols), count)
    taps_ref[inner, 0:channels] = left.astype(jnp.bfloat16)
    taps_ref[inner, channels : 2 * channels] = block.astype(jnp.bfloat16)
    taps_ref[inner, 2 * channels :] = right.astype(jnp.bfloat16)


def clear_edges(taps_ref, cols):
    edge = jnp.zeros((cols, taps_ref.shape[1]), taps_ref.dtype)
    taps_ref[0:cols, :] = edge
    taps_ref[taps_ref.shape[0] - cols :, :] = edge


def begin_conv(taps_ref, product, total_ref, fill, first, cols):
    for start in range(0, total_ref.shape[0], FILL_ROWS):
        for inner in range(start, start + FILL_ROWS, CHUNK):
            fill(pl.ds(inner, CHUNK))
        rows = pl.ds(start, FILL_ROWS)
        total_ref[rows, :] = first(rows, product(taps_ref, pl.ds(start + cols, FILL_ROWS), 1))


def add_rows(taps_ref, product, mask_ref, total_ref, row_tap, last, cols, old_ref=None):
    pixels, channels = total_ref.shape
    old_ref = total_ref if old_ref is None else old_ref
    for start in range(0, pixels, FILL_ROWS):
        rows = slice(start, start + FILL_ROWS)
        part = product(taps_ref, pl.ds(start + row_tap * cols, FILL_ROWS), row_tap)
        mask = widen(mask_ref[row_tap // 2, rows, :], channels)
        total_ref[rows, :] = last(rows, old_ref[rows, :] + mask * part)


def run_conv(taps_ref, product, mask_ref, total_ref, fill, first, last, cols):
    begin_conv(taps_ref, product, total_ref, fill, first, cols)
    add_rows(taps_ref, product, mask_ref, total_ref, 0, lambda rows, value: value, cols)
    add_rows(taps_ref, product, mask_ref, total_ref, 2, last, cols)


def product_forward(weight_ref):
    channels = weight_ref.shape[-1]

    def product(taps_ref, shifted, row_tap):
        return jnp.dot(
            taps_ref[shifted, :],
            weight_ref[row_tap].reshape(3 * channels, channels),
            preferred_element_type=jnp.float32,
        )

    return product


def product_backward(weight_ref):
    def product(taps_ref, shifted, row_tap):
        return lax.dot_general(
            taps_ref[shifted, :],
            weight_ref[row_tap],
            (((1,), (1,)), ((), ())),
            preferred_element_type=jnp.float32,
        )

    return product


def smooth(values):
    part = 0.5 * jnp.tanh(0.5 * values) + 0.5
    return values * part, part


def activation(read, mean, inverse, gain, shift, act_ref, taps_ref, cols):
    scale = inverse * gain

    def fill(rows):
        act = smooth((read(rows) - mean) * scale + shift)[0]
        act_ref[rows, :] = act.astype(jnp.bfloat16)
        put_taps(taps_ref, act, rows, cols)

    return fill


def back_means(sums, gain, pixels):
    channels = gain.shape[1]
    members = float(pixels * (channels // GROUPS))
    return group_mean(sums[0] * gain, members), group_mean(sums[1] * gain, members)


def column_total(partial):
    return jnp.sum(partial, axis=0, keepdims=True)


def weight_part(act_ref, grad_ref, lanes_ref, flip_ref, columns_ref, part_ref, cols):
    pixels, channels = act_ref.shape
    height = lax.axis_index("height")
    share = NARROW // 2
    block = pl.ds(pl.multiple_of((height // 2) * NARROW, NARROW), NARROW)
    flip_ref[...] = grad_ref[:, block].T
    own = pl.ds(pl.multiple_of((height % 2) * share, share), share)
    grad = flip_ref[own, :].astype(jnp.float32)
    column = lax.broadcasted_iota(jnp.int32, grad.shape, 1) & (cols - 1)
    for col_tap in range(3):
        shifted = grad
        if col_tap == 0:
            shifted = jnp.where(column == cols - 1, 0.0, pltpu.roll(grad, pixels - 1, 1))
        elif col_tap == 2:
            shifted = jnp.where(column == 0, 0.0, pltpu.roll(grad, 1, 1))
        for row_tap in range(3):
            tap = 3 * row_tap + col_tap
            place = slice(tap * share, (tap + 1) * share)
            if row_tap == 1:
                columns_ref[place, :] = shifted.astype(jnp.bfloat16)
                continue
            side, turn = (0, pixels - cols) if row_tap == 0 else (1, cols)
            masked = (shifted * lanes_ref[side : side + 1, :]).astype(jnp.bfloat16)
            columns_ref[place, :] = pltpu.roll(masked, turn, 1)
    part_ref[...] = jnp.dot(
        columns_ref[...], act_ref[...], preferred_element_type=jnp.float32
    ).astype(jnp.bfloat16)


def begin_back(grad_ref, weights_ref, mask_ref, taps_ref, total_ref, cols):
    clear_edges(taps_ref, cols)

    def fill(rows):
        put_taps(taps_ref, grad_ref[rows, :].astype(jnp.float32), rows, cols)

    product = product_backward(weights_ref)
    begin_conv(taps_ref, product, total_ref, fill, lambda rows, part: part, cols)
    add_rows(taps_ref, product, mask_ref, total_ref, 0, lambda rows, value: value, cols)


def finish_back(
    weights_ref, mask_ref, taps_ref, total_ref, read, table_ref, which, cols, old_ref=None
):
    mean, inverse, gain, shift = norm_rows(table_ref, which)
    sums = []

    def slope(rows, value):
        normed = (read(rows) - mean) * inverse
        pre = normed * gain + shift
        part = smooth(pre)[1]
        grad = value * (part * (1.0 + pre * (1.0 - part)))
        sums.append((fold(grad), fold(grad * normed)))
        return grad

    add_rows(
        taps_ref, product_backward(weights_ref), mask_ref, total_ref, 2, slope, cols, old_ref
    )
    return sum(pair[0] for pair in sums), sum(pair[1] for pair in sums)


def norm_back(total_ref, sums, read, table_ref, which):
    mean, inverse, gain, shift = norm_rows(table_ref, which)
    mean_grad, mean_cross = back_means(sums, gain, total_ref.shape[0])

    def back(rows):
        normed = (read(rows) - mean) * inverse
        return inverse * (total_ref[rows, :] * gain - mean_grad - normed * mean_cross)

    return back


def turn_kernel(
    grad_ref, mask_ref, weights_ref, middle_ref, table_ref, total_ref, sums_ref, taps_ref, *, cols
):
    begin_back(grad_ref, weights_ref.at[1], mask_ref, taps_ref, total_ref, cols)
    sums_ref[0:8, :], sums_ref[8:16, :] = finish_back(
        weights_ref.at[1],
        mask_ref,
        taps_ref,
        total_ref,
        lambda rows: middle_ref[rows, :],
        table_ref,
        1,
        cols,
    )


def norm_rows(table_ref, which):
    picks = (2 * which, 2 * which + 1, 6 + which, 9 + which)
    return tuple(table_ref[pick : pick + 1, :] for pick in picks)


def build_masks(ids_ref, mask_ref, lanes_ref, id_rows_ref, id_cols_ref, cols):
    rows = ids_ref.shape[1]
    for row in range(rows):
        here = ids_ref[0, row]
        place = slice(row * cols, (row + 1) * cols)
        id_rows_ref[place, :] = jnp.full((cols, LANES), here, jnp.int32)
        for side, other in ((0, row - 1), (1, row + 1)):
            same = jnp.float32(0.0)
            if 0 <= other < rows:
                same = jnp.where(ids_ref[0, other] == here, 1.0, 0.0).astype(jnp.float32)
            mask_ref[side, place, :] = jnp.full((cols, LANES), same, jnp.float32)
    lane = lax.broadcasted_iota(jnp.int32, (8, LANES), 1)
    each = LANES // cols
    for block in range(rows // each):
        ids = jnp.full((8, LANES), ids_ref[0, block * each], jnp.int32)
        for step in range(1, each):
            ids = jnp.where(lane >= step * cols, ids_ref[0, block * each + step], ids)
        id_cols_ref[:, block * LANES : (block + 1) * LANES] = ids
    ids = id_cols_ref[...].astype(jnp.float32)
    pixels = ids.shape[1]
    pixel = lax.broadcasted_iota(jnp.int32, ids.shape, 1)
    above = jnp.where(pixel < cols, -1.0, pltpu.roll(ids, cols, 1))
    below = jnp.where(pixel >= pixels - cols, -1.0, pltpu.roll(ids, pixels - cols, 1))
    lanes_ref[0:1, :] = jnp.where(above == ids, 1.0, 0.0)[0:1]
    lanes_ref[1:2, :] = jnp.where(below == ids, 1.0, 0.0)[0:1]


def place_pieces(pieces, whole_ref, sems):
    own_pixels = whole_ref.shape[0] // len(pieces)
    height = lax.axis_index("height")
    copies = []
    for place, piece in enumerate(pieces):
        start = pl.multiple_of((height ^ place) * own_pixels, own_pixels)
        rows = pl.ds(start, own_pixels)
        copies.append(pltpu.make_async_copy(piece, whole_ref.at[rows, :], sems.at[place]))
    return copies


def hold_kernel(
    ids_hbm,
    gains_hbm,
    shifts_hbm,
    biases_hbm,
    weights_hbm,
    qkv_hbm,
    proj_hbm,
    qv_bias_hbm,
    proj_bias_hbm,
    weights_ref,
    turned_ref,
    qkv_ref,
    proj_ref,
    table_ref,
    mask_ref,
    lanes_ref,
    id_rows_ref,
    id_cols_ref,
    ids_ref,
    gains_ref,
    shifts_ref,
    biases_ref,
    qv_bias_ref,
    proj_bias_ref,
    sems,
    *,
    cols,
):
    channels = weights_ref.shape[-1]
    small = [
        (ids_hbm, ids_ref),
        (gains_hbm, gains_ref),
        (shifts_hbm, shifts_ref),
        (biases_hbm, biases_ref),
        (qv_bias_hbm, qv_bias_ref),
        (proj_bias_hbm, proj_bias_ref),
    ]
    large = [(weights_hbm, weights_ref), (qkv_hbm, qkv_ref), (proj_hbm, proj_ref)]
    for which in range(2):
        for row_tap in range(3):
            for col_tap in range(3):
                place = slice(col_tap * channels, (col_tap + 1) * channels)
                large.append(
                    (
                        weights_hbm.at[which, 2 - row_tap, 2 - col_tap],
                        turned_ref.at[which, row_tap, :, place],
                    )
                )
    copies = [
        pltpu.make_async_copy(source, target, sems.at[index])
        for index, (source, target) in enumerate(small + large)
    ]
    for copy in copies:
        copy.start()
    for copy in copies[: len(small)]:
        copy.wait()
    build_masks(ids_ref, mask_ref, lanes_ref, id_rows_ref, id_cols_ref, cols)
    table_ref[6:9, :] = gains_ref[...]
    table_ref[9:12, :] = shifts_ref[...]
    table_ref[12:14, :] = biases_ref[...]
    table_ref[14:16, :] = qv_bias_ref[...]
    table_ref[16:17, :] = proj_bias_ref[...]
    for copy in copies[len(small) :]:
        copy.wait()


def conv_kernel(*refs, cols, count):
    pieces, refs = refs[:count], refs[count:]
    (
        weights_ref,
        params_ref,
        mask_ref,
        features_ref,
        act_one_ref,
        middle_ref,
        act_two_ref,
        residual_ref,
        table_ref,
        own_ref,
        taps_ref,
        sem,
    ) = refs
    pixels, channels = features_ref.shape
    wide = jnp.float32
    own_copy = pltpu.make_async_copy(pieces[0], own_ref, sem)
    own_copy.start()
    table_ref[...] = params_ref[...]
    clear_edges(taps_ref, cols)

    def read_input(rows):
        return features_ref[rows, :].astype(wide)

    def read_middle(rows):
        return middle_ref[rows, :]

    height = lax.axis_index("height")
    own_pixels = pixels // count
    seen = RunningStats(channels)
    for place in list(range(1, count)) + [0]:
        if place == 0:
            own_copy.wait()
        piece = (pieces[place] if place else own_ref)[...]
        start = pl.multiple_of((height ^ place) * own_pixels, own_pixels)
        features_ref[pl.ds(start, own_pixels), :] = piece
        seen.add(piece.astype(wide))
    table_ref[0:1, :], table_ref[1:2, :] = seen.finish(pixels)
    seen = RunningStats(channels)

    def keep(rows, value):
        seen.add(value)
        return value

    run_conv(
        taps_ref,
        product_forward(weights_ref.at[0]),
        mask_ref,
        middle_ref,
        activation(read_input, *norm_rows(table_ref, 0), act_one_ref, taps_ref, cols),
        lambda rows, part: part + table_ref[12:13, :],
        keep,
        cols,
    )
    table_ref[2:3, :], table_ref[3:4, :] = seen.finish(pixels)
    seen = RunningStats(channels)
    run_conv(
        taps_ref,
        product_forward(weights_ref.at[1]),
        mask_ref,
        residual_ref,
        activation(read_middle, *norm_rows(table_ref, 1), act_two_ref, taps_ref, cols),
        lambda rows, part: part + (read_input(rows) + table_ref[13:14, :]),
        keep,
        cols,
    )
    table_ref[4:5, :], table_ref[5:6, :] = seen.finish(pixels)


def score_kernel(
    qkv_ref,
    proj_ref,
    residual_ref,
    table_ref,
    id_rows_ref,
    id_cols_ref,
    normed_ref,
    query_ref,
    key_ref,
    value_ref,
    soft_ref,
    out_flip_ref,
    output_ref,
    value_flip_ref,
    *,
    score_scale,
):
    pixels, channels = residual_ref.shape
    own_pixels = output_ref.shape[0]
    wide = jnp.float32
    exponent = score_scale * 1.4426950408889634
    mean, inverse, gain, shift = norm_rows(table_ref, 2)
    scale = inverse * gain
    block = min(QUERY_ROWS, pixels)

    def project(rows, carry):
        normed = ((residual_ref[rows, :] - mean) * scale + shift).astype(jnp.bfloat16)
        normed_ref[rows, :] = normed
        query_ref[rows, :] = (
            jnp.dot(normed, qkv_ref[:, 0:channels], preferred_element_type=wide)
            + table_ref[14:15, :]
        ).astype(jnp.bfloat16)
        key_ref[rows, :] = jnp.dot(
            normed, qkv_ref[:, channels : 2 * channels], preferred_element_type=wide
        ).astype(jnp.bfloat16)
        values = (
            jnp.dot(normed, qkv_ref[:, 2 * channels :], preferred_element_type=wide)
            + table_ref[15:16, :]
        ).astype(jnp.bfloat16)
        value_ref[rows, :] = values
        value_flip_ref[:, rows] = values.T
        return carry

    each_block(pixels, block, project)

    def attend(rows, carry):
        scores = lax.dot_general(
            key_ref[...], query_ref[rows, :], (((1,), (1,)), ((), ())), preferred_element_type=wide
        )
        same = widen(id_rows_ref[...], block) == id_cols_ref[0:1, rows]
        scores = jnp.where(same, scores, masked_score)
        scores = jnp.exp2((scores - jnp.max(scores, axis=0, keepdims=True)) * exponent)
        weights = scores * (1.0 / jnp.sum(scores, axis=0, keepdims=True))
        soft_ref[:, rows] = weights.astype(jnp.bfloat16)
        return carry

    each_block(pixels, block, attend)

    def collect(rows, carry):
        out_flip_ref[rows, :] = jnp.dot(
            value_flip_ref[rows, :], soft_ref[...], preferred_element_type=wide
        ).astype(jnp.bfloat16)
        return carry

    each_block(channels, channels // 2, collect)
    height = lax.axis_index("height")
    own = pl.ds(pl.multiple_of(height * own_pixels, own_pixels), own_pixels)
    output_ref[...] = (
        residual_ref[own, :]
        + lax.dot_general(
            out_flip_ref[:, own],
            proj_ref[...],
            (((0,), (0,)), ((), ())),
            preferred_element_type=wide,
        )
        + table_ref[16:17, :]
    ).astype(jnp.bfloat16)


def own_quarter():
    height = lax.axis_index("height")
    return (height & 1) * 2 + ((height >> 1) & 1)


def send_order(source_ref, targets, axis, share):
    me = lax.axis_index("canvas")
    for step, target in enumerate(targets):
        place = pl.ds(pl.multiple_of((me ^ step) * share, share), share)
        target[...] = source_ref[place, :] if axis == 0 else source_ref[:, place]


def attention_kernel(
    proj_ref,
    normed_ref,
    query_ref,
    key_ref,
    value_ref,
    soft_ref,
    out_flip_ref,
    *refs,
    score_scale,
    count,
):
    pieces, (grad_ref, packed_ref, sums_ref), refs = (
        refs[:count],
        refs[count : count + 3],
        refs[count + 3 :],
    )
    *mixed_refs, mixed_ref, key_flip_ref, back_ref, score_grad_ref, flip_ref, sems = refs
    pixels, channels = normed_ref.shape
    block = min(QUERY_ROWS, pixels)
    wide = jnp.float32
    copies = place_pieces(pieces, grad_ref, sems)
    for copy in copies:
        copy.start()
    quarter = channels // 4
    own = pl.ds(pl.multiple_of(own_quarter() * quarter, quarter), quarter)
    flip_ref[...] = normed_ref[:, own].T
    key_flip_ref[...] = key_ref[...].T
    for copy in copies:
        copy.wait()

    for start in range(0, pixels, block):
        rows = slice(start, start + block)
        back_ref[rows, :] = lax.dot_general(
            grad_ref[rows, :], proj_ref[...], (((1,), (1,)), ((), ())), preferred_element_type=wide
        ).astype(jnp.bfloat16)
    for start in range(0, pixels, block):
        rows = slice(start, start + block)
        weights = soft_ref[:, rows].astype(wide)
        weight_grad = lax.dot_general(
            value_ref[...],
            back_ref[rows, :],
            (((1,), (1,)), ((), ())),
            preferred_element_type=wide,
        )
        dots = jnp.sum(weights * weight_grad, axis=0, keepdims=True)
        score_grad = (weights * (weight_grad - dots)).astype(jnp.bfloat16)
        score_grad_ref[:, rows] = score_grad
        query_grad = jnp.dot(key_flip_ref[...], score_grad, preferred_element_type=wide)
        packed_ref[rows, 0:channels] = (query_grad * score_scale).astype(jnp.bfloat16).T
        packed_ref[rows, 2 * channels :] = jnp.dot(
            soft_ref[rows, :], back_ref[...], preferred_element_type=wide
        ).astype(jnp.bfloat16)
    for start in range(0, pixels, block):
        rows = slice(start, start + block)
        packed_ref[rows, channels : 2 * channels] = (
            jnp.dot(score_grad_ref[rows, :], query_ref[...], preferred_element_type=wide)
            * score_scale
        ).astype(jnp.bfloat16)

    def pack(rows, carry):
        return (
            carry[0] + fold(packed_ref[rows, 0:channels].astype(wide)),
            carry[1] + fold(packed_ref[rows, 2 * channels :].astype(wide)),
            carry[2] + fold(grad_ref[rows, :].astype(wide)),
        )

    zeros = jnp.zeros((8, channels), wide)
    totals = zeros, zeros, zeros
    for start in range(0, pixels, CHUNK):
        totals = pack(pl.ds(start, CHUNK), totals)
    sums_ref[...] = jnp.zeros(sums_ref.shape, wide)
    for row, total in enumerate(totals):
        sums_ref[8 + row : 9 + row, :] = column_total(total)
    mixed_ref[:, 0 : 3 * channels] = jnp.dot(
        flip_ref[...], packed_ref[...], preferred_element_type=wide
    ).astype(jnp.bfloat16)
    mixed_ref[:, 3 * channels :] = jnp.dot(
        out_flip_ref[own, :], grad_ref[...], preferred_element_type=wide
    ).astype(jnp.bfloat16)
    send_order(mixed_ref, mixed_refs, 0, quarter // len(mixed_refs))


def third_kernel(
    qkv_ref,
    grad_ref,
    packed_ref,
    residual_ref,
    table_ref,
    act_two_ref,
    lanes_ref,
    old_sums_ref,
    residual_grad_ref,
    grad_two_ref,
    sums_ref,
    keep_ref,
    send_ref,
    total_ref,
    flip_ref,
    columns_ref,
    part_ref,
    *,
    cols,
):
    pixels, channels = residual_ref.shape
    block = FILL_ROWS
    wide = jnp.float32
    mean, inverse, gain, shift = norm_rows(table_ref, 2)
    zeros = jnp.zeros((8, channels), wide)

    sums = (zeros, zeros)
    for start in range(0, pixels, block):
        rows = pl.ds(start, block)
        normed_grad = lax.dot_general(
            packed_ref[rows, :], qkv_ref[...], (((1,), (1,)), ((), ())), preferred_element_type=wide
        )
        total_ref[rows, :] = normed_grad
        normed = (residual_ref[rows, :] - mean) * inverse
        sums = sums[0] + fold(normed_grad), sums[1] + fold(normed_grad * normed)
    sums_ref[...] = old_sums_ref[...]
    sums_ref[5:6, :] = column_total(sums[1])
    sums_ref[6:7, :] = column_total(sums[0])
    mean_grad, mean_cross = back_means(sums, gain, pixels)

    def finish(rows, carry):
        normed = (residual_ref[rows, :] - mean) * inverse
        back = inverse * (total_ref[rows, :] * gain - mean_grad - normed * mean_cross)
        total = grad_ref[rows, :].astype(wide) + back
        residual_grad_ref[rows, :] = total
        low = total.astype(jnp.bfloat16)
        grad_two_ref[rows, :] = low
        return carry + fold(low.astype(wide))

    sums_ref[7:8, :] = column_total(each_chunk(pixels, finish, zeros))
    weight_part(act_two_ref, grad_two_ref, lanes_ref, flip_ref, columns_ref, part_ref, cols)
    keep_half(part_ref, 2, 1, keep_ref, send_ref)


def second_kernel(
    total_ref,
    partial_ref,
    middle_ref,
    table_ref,
    act_one_ref,
    lanes_ref,
    old_sums_ref,
    grad_one_ref,
    sums_ref,
    keep_ref,
    send_ref,
    flip_ref,
    columns_ref,
    part_ref,
    *,
    cols,
):
    pixels, channels = middle_ref.shape
    sums = partial_ref[0:8, :], partial_ref[8:16, :]
    back = norm_back(total_ref, sums, lambda rows: middle_ref[rows, :], table_ref, 1)
    sums_ref[...] = old_sums_ref[...]
    sums_ref[2:3, :] = column_total(sums[1])
    sums_ref[3:4, :] = column_total(sums[0])

    def finish(rows, carry):
        low = back(rows).astype(jnp.bfloat16)
        grad_one_ref[rows, :] = low
        return carry + fold(low.astype(jnp.float32))

    zeros = jnp.zeros((8, channels), jnp.float32)
    sums_ref[4:5, :] = column_total(each_chunk(pixels, finish, zeros))
    weight_part(act_one_ref, grad_one_ref, lanes_ref, flip_ref, columns_ref, part_ref, cols)
    keep_half(part_ref, 1, 2, keep_ref, send_ref)


def keep_half(part_ref, near, far, keep_ref, send_ref):
    me = lax.axis_index("canvas")
    rows, width = part_ref.shape[0], keep_ref.shape[1]
    for target_ref, flip in ((keep_ref, 0), (send_ref, near)):
        for slot in range(2):
            owner = me ^ flip ^ (slot * far)
            place = pl.ds(pl.multiple_of(owner * width, width), width)
            target_ref[slot * rows : (slot + 1) * rows, :] = part_ref[:, place]


def begin_kernel(grad_ref, mask_ref, weights_ref, total_ref, taps_ref, *, cols):
    begin_back(grad_ref, weights_ref.at[0], mask_ref, taps_ref, total_ref, cols)


def first_kernel(
    old_total_ref,
    taps_ref,
    features_ref,
    table_ref,
    mask_ref,
    old_sums_ref,
    weights_ref,
    own_ref,
    sums_ref,
    partial_ref,
    total_ref,
    *,
    cols,
):
    def read(rows):
        return features_ref[rows, :].astype(jnp.float32)

    sums = finish_back(
        weights_ref.at[0],
        mask_ref,
        taps_ref,
        total_ref,
        read,
        table_ref,
        0,
        cols,
        old_total_ref,
    )
    partial_ref[0:8, :], partial_ref[8:16, :] = sums
    sums_ref[...] = old_sums_ref[...]
    sums_ref[0:1, :] = column_total(sums[1])
    sums_ref[1:2, :] = column_total(sums[0])
    count = own_ref.shape[0]
    own = pl.ds(pl.multiple_of(lax.axis_index("height") * count, count), count)
    own_ref[...] = total_ref[own, :]


def own_kernel(
    own_ref,
    partial_ref,
    features_ref,
    residual_grad_ref,
    table_ref,
    packed_ref,
    old_qkv,
    old_proj,
    input_grad_ref,
    qkv_hbm,
    proj_hbm,
    qkv_ref,
    proj_ref,
    sems,
):
    copies = spread_quarters([packed_ref], [2], qkv_ref, proj_ref, qkv_hbm, proj_hbm, sems)
    mean, inverse, gain, shift = norm_rows(table_ref, 0)
    pixels = features_ref.shape[0]
    sums = partial_ref[0:8, :], partial_ref[8:16, :]
    mean_grad, mean_cross = back_means(sums, gain, pixels)
    count = own_ref.shape[0]
    own = pl.ds(pl.multiple_of(lax.axis_index("height") * count, count), count)
    normed = (features_ref[own, :].astype(jnp.float32) - mean) * inverse
    back = inverse * (own_ref[...] * gain - mean_grad - normed * mean_cross)
    input_grad_ref[...] = (residual_grad_ref[own, :] + back).astype(jnp.bfloat16)
    for copy in copies:
        copy.wait()


def place_kernel(*refs):
    joints, (qkv_hbm, proj_hbm, packed_ref, qkv_ref, proj_ref, sems) = refs[:-6], refs[-6:]
    share = packed_ref.shape[0] // len(joints)
    me = lax.axis_index("canvas")
    for step, joint in enumerate(joints):
        place = pl.ds(pl.multiple_of((me ^ step) * share, share), share)
        packed_ref[place, :] = joint[...]
    copies = spread_quarters([packed_ref], [0], qkv_ref, proj_ref, qkv_hbm, proj_hbm, sems)
    for copy in copies:
        copy.wait()


def spread_quarters(packed, flips, qkv_ref, proj_ref, qkv_hbm, proj_hbm, sems):
    quarter = packed[0].shape[0]
    inner = qkv_ref.shape[2]
    copies = []
    for index, packed_ref in enumerate(packed):
        owner = own_quarter() ^ flips[index]
        rows = pl.ds(pl.multiple_of(owner * quarter, quarter), quarter)
        qkv_ref[index] = packed_ref[:, 0:inner].astype(jnp.float32)
        proj_ref[index] = packed_ref[:, inner:].astype(jnp.float32)
        for which, (held, target) in enumerate(((qkv_ref, qkv_hbm), (proj_ref, proj_hbm))):
            copy = pltpu.make_async_copy(held.at[index], target.at[rows, :], sems.at[index, which])
            copy.start()
            copies.append(copy)
    return copies


def join_kernel(
    old_qkv, old_proj, chip_ref, both_ref, qkv_hbm, proj_hbm, qkv_ref, proj_ref, sems
):
    copies = spread_quarters(
        [chip_ref, both_ref], [1, 3], qkv_ref, proj_ref, qkv_hbm, proj_hbm, sems
    )
    for copy in copies:
        copy.wait()


def halve_kernel(keep_ref, got_ref, hold_ref, send_ref):
    total = keep_ref[...].astype(jnp.float32) + got_ref[...].astype(jnp.float32)
    rows = hold_ref.shape[0]
    hold_ref[...] = total[0:rows]
    send_ref[...] = total[rows:].astype(jnp.bfloat16)


def sums_kernel(
    sums_ref,
    got_sums_ref,
    hold_one_ref,
    got_one_ref,
    hold_two_ref,
    got_two_ref,
    share_ref,
    gains_ref,
    shifts_ref,
    conv_ref,
    qv_ref,
    proj_ref,
):
    for which, (hold_ref, got_ref) in enumerate(
        ((hold_one_ref, got_one_ref), (hold_two_ref, got_two_ref))
    ):
        total = hold_ref[...] + got_ref[...].astype(jnp.float32)
        share_ref[which] = total.reshape(share_ref.shape[1:])
    total = sums_ref[...] + got_sums_ref[...]
    for row, start in enumerate((0, 2, 5)):
        gains_ref[row : row + 1, :] = total[start : start + 1]
        shifts_ref[row : row + 1, :] = total[start + 1 : start + 2]
    conv_ref[0:1, :] = total[4:5]
    conv_ref[1:2, :] = total[7:8]
    qv_ref[...] = total[8:10]
    proj_ref[...] = total[10:11]


def call_kernel(kernel, outputs, scratch, operands, places, flops, limit, out_places=None, aliases={}):
    out_places = out_places or "v" * len(outputs)
    spaces = {
        "v": pl.BlockSpec(memory_space=pltpu.VMEM),
        "s": pl.BlockSpec(memory_space=pltpu.SMEM),
        "h": pl.BlockSpec(memory_space=pl.ANY),
        "o": pl.BlockSpec(memory_space=pltpu.VMEM),
        "a": pl.BlockSpec(memory_space=pl.ANY),
    }
    moved = 8 * flops // LANES
    held = {"v": pltpu.VMEM, "h": pltpu.HBM, "o": jax.ShapeDtypeStruct}
    operands = [
        pltpu.with_memory_space_constraint(array, pltpu.HBM) if place == "h" else array
        for array, place in zip(operands, places)
    ]
    return pl.pallas_call(
        kernel,
        out_shape=[held[place](*output) for output, place in zip(outputs, out_places)],
        in_specs=[spaces[place] for place in places],
        out_specs=[spaces[place] for place in out_places],
        scratch_shapes=scratch,
        input_output_aliases=aliases,
        compiler_params=pltpu.CompilerParams(vmem_limit_bytes=limit * 2**20),
        cost_estimate=pl.CostEstimate(flops=flops, bytes_accessed=moved, transcendentals=0),
    )(*operands)


def send_height(block, step):
    size = lax.axis_size("height")
    return lax.ppermute(block, "height", [(i, i ^ step) for i in range(size)])


def with_cores(blocks):
    return [piece for block in blocks for piece in (block, send_height(block, 1))]


def send_canvas(block, step):
    size = lax.axis_size("canvas")
    return lax.ppermute(block, "canvas", [(i, i ^ step) for i in range(size)])


def trade_canvas(pieces):
    return [pieces[0]] + [send_canvas(piece, step) for step, piece in enumerate(pieces) if step]


def whole_canvas(
    features,
    tile_ids,
    norm_gains,
    norm_shifts,
    conv_weights,
    conv_biases,
    qkv_weight,
    qv_bias,
    proj_weight,
    proj_bias,
    cotangent,
):
    height_size = lax.axis_size("height")
    canvas_size = lax.axis_size("canvas")
    local_rows, cols, channels = features.shape[1:]
    all_rows = tile_ids.shape[1]
    pixels = all_rows * cols
    own_pixels = local_rows * cols
    out_share = channels // height_size
    ci_share = channels // canvas_size
    quarter = channels // 4
    row_share = quarter // canvas_size
    low, wide = jnp.bfloat16, jnp.float32

    own_features = features.reshape(own_pixels, channels)
    own_grad = cotangent.reshape(own_pixels, channels)
    steps = range(2, height_size, 2)
    held_features = [own_features] + [send_height(own_features, step) for step in steps]
    plane = ((pixels, channels), low)
    plane_wide = ((pixels, channels), wide)
    sums_shape = ((16, channels), wide)
    mixed_shapes = [((row_share, 4 * channels), low)] * canvas_size
    taps = pltpu.VMEM((pixels + 2 * cols, 3 * channels), low)
    held_wide = pltpu.VMEM((pixels, channels), wide)
    flipped = pltpu.VMEM((channels, pixels), low)
    narrow = pltpu.VMEM((NARROW, pixels), low)
    columns = pltpu.VMEM((9 * out_share, pixels), low)
    part_held = pltpu.VMEM((9 * out_share, channels), low)
    sem = pltpu.SemaphoreType.DMA
    conv_flops = 2 * 9 * pixels * channels * channels
    dot_flops = 2 * pixels * channels * channels
    score_flops = 2 * pixels * pixels * channels
    scale = channels ** (-0.5)

    (
        held_conv,
        turned,
        held_qkv,
        held_proj,
        params,
        mask,
        lane_mask,
        id_rows,
        id_cols,
    ) = call_kernel(
        functools.partial(hold_kernel, cols=cols),
        [
            (conv_weights.shape, low),
            ((2, 3, channels, 3 * channels), low),
            (qkv_weight.shape, low),
            (proj_weight.shape, low),
            ((24, channels), wide),
            ((2, pixels, LANES), wide),
            ((8, pixels), wide),
            ((pixels, LANES), jnp.int32),
            ((8, pixels), jnp.int32),
        ],
        [
            pltpu.SMEM(tile_ids.shape, jnp.int32),
            pltpu.VMEM(norm_gains.shape, wide),
            pltpu.VMEM(norm_shifts.shape, wide),
            pltpu.VMEM(conv_biases.shape, wide),
            pltpu.VMEM(qv_bias.shape, wide),
            pltpu.VMEM((1, channels), wide),
            sem((27,)),
        ],
        [
            tile_ids,
            norm_gains,
            norm_shifts,
            conv_biases,
            conv_weights,
            qkv_weight,
            proj_weight,
            qv_bias,
            proj_bias.reshape(1, channels),
        ],
        "h" * 9,
        conv_flops,
        8,
    )
    held_features[1:] = [
        lax.optimization_barrier((params, block))[1] for block in held_features[1:]
    ]
    pieces = with_cores(held_features)
    far_grad, *pieces[4::2] = lax.optimization_barrier((own_grad, *held_features[2:]))
    held_grads = [own_grad, send_height(own_grad, 2)]
    held_grads[1], pieces[2] = lax.optimization_barrier((held_grads[1], held_features[1]))
    held_grads += [send_height(far_grad, step) for step in steps[1:]]

    all_features, act_one, middle, act_two, residual, table = call_kernel(
        functools.partial(conv_kernel, cols=cols, count=height_size),
        [plane, plane, plane_wide, plane, plane_wide, ((24, channels), wide)],
        [pltpu.VMEM((own_pixels, channels), low), taps, sem],
        [*pieces, held_conv, params, mask],
        "h" + "v" * (height_size + 2),
        2 * conv_flops,
        16,
    )
    residual, *held_grads = lax.optimization_barrier((residual, *held_grads))
    grad_pieces = with_cores(held_grads)
    normed, query, key, value, soft, out_flip, output = call_kernel(
        functools.partial(score_kernel, score_scale=scale),
        [
            plane,
            plane,
            plane,
            plane,
            ((pixels, pixels), low),
            ((channels, pixels), low),
            ((own_pixels, channels), low),
        ],
        [
            flipped,
        ],
        [
            held_qkv,
            held_proj,
            residual,
            table,
            id_rows,
            id_cols,
        ],
        "vvvvvv",
        3 * dot_flops + 2 * score_flops,
        16,
        "v" * 6 + "o",
    )
    normed, *grad_pieces = lax.optimization_barrier((normed, *grad_pieces))
    all_grad, packed, sums, *mixed = call_kernel(
        functools.partial(attention_kernel, score_scale=scale, count=height_size),
        [plane, ((pixels, 3 * channels), low), sums_shape, *mixed_shapes],
        [
            pltpu.VMEM((quarter, 4 * channels), low),
            flipped,
            pltpu.VMEM((pixels, channels), low),
            pltpu.VMEM((pixels, pixels), low),
            pltpu.VMEM((quarter, pixels), low),
            sem((height_size,)),
        ],
        [held_proj, normed, query, key, value, soft, out_flip, *grad_pieces],
        "vvvvvvvh" + "a" * (height_size - 1),
        3 * dot_flops + 4 * score_flops,
        20,
    )
    mixed = trade_canvas(mixed)
    halves = [((18 * out_share, ci_share), low)] * 2
    residual_grad, grad_two, sums, keep_two, send_two = call_kernel(
        functools.partial(third_kernel, cols=cols),
        [plane_wide, plane, sums_shape, *halves],
        [held_wide, narrow, columns, part_held],
        [held_qkv, all_grad, packed, residual, table, act_two, lane_mask, sums],
        "vvvvvvvv",
        3 * dot_flops + conv_flops // height_size,
        16,
    )
    grad_two, *mixed = lax.optimization_barrier((grad_two, *mixed))
    mixed_sum = mixed[0].astype(wide)
    for piece in mixed[1:]:
        mixed_sum = mixed_sum + piece.astype(wide)
    joints = trade_canvas([mixed_sum.astype(low)] * canvas_size)
    act_two_grad, partial_sums = call_kernel(
        functools.partial(turn_kernel, cols=cols),
        [plane_wide, sums_shape],
        [taps],
        [grad_two, mask, turned, middle, table],
        "vvvvv",
        conv_flops,
        16,
    )
    act_two_grad, *joints = lax.optimization_barrier((act_two_grad, *joints))
    qkv_grad, proj_grad, own_mixed = call_kernel(
        place_kernel,
        [(qkv_weight.shape, wide), (proj_weight.shape, wide), ((quarter, 4 * channels), low)],
        [
            pltpu.VMEM((1, quarter, 3 * channels), wide),
            pltpu.VMEM((1, quarter, channels), wide),
            sem((1, 2)),
        ],
        joints,
        "v" * canvas_size,
        0,
        12,
        "hhv",
    )
    own_mixed, send_two = lax.optimization_barrier((own_mixed, send_two))
    got_two = send_canvas(send_two, 2)
    chip_mixed = send_height(own_mixed, 2)
    core_mixed = send_height(own_mixed, 1)
    grad_one, sums, keep_one, send_one = call_kernel(
        functools.partial(second_kernel, cols=cols),
        [plane, sums_shape, *halves],
        [narrow, columns, part_held],
        [act_two_grad, partial_sums, middle, table, act_one, lane_mask, sums],
        "vvvvvvv",
        1,
        16,
    )
    got_one = send_canvas(send_one, 1)

    def halve(keep, got):
        return call_kernel(
            halve_kernel,
            [((9 * out_share, ci_share), kind) for kind in (wide, low)],
            [],
            [keep, got],
            "vv",
            0,
            12,
        )

    half_total, half_taps = call_kernel(
        functools.partial(begin_kernel, cols=cols),
        [plane_wide, (taps.shape, low)],
        [],
        [grad_one, mask, turned],
        "vvv",
        1,
        16,
    )
    half_total, got_two = lax.optimization_barrier((half_total, got_two))
    hold_two, send_two = halve(keep_two, got_two)
    got_two = send_canvas(send_two, 1)
    half_total, hold_two = lax.optimization_barrier((half_total, hold_two))
    own_total, sums, partial_sums = call_kernel(
        functools.partial(first_kernel, cols=cols),
        [((own_pixels, channels), wide), sums_shape, sums_shape],
        [held_wide],
        [half_total, half_taps, all_features, table, mask, sums, turned],
        "vvvvvvv",
        conv_flops // 3,
        16,
    )
    sums, core_mixed, got_one = lax.optimization_barrier((sums, core_mixed, got_one))
    got_sums = send_canvas(sums, 1)
    hold_one, send_one = halve(keep_one, got_one)
    got_one = send_canvas(send_one, 2)
    own_total, hold_one = lax.optimization_barrier((own_total, hold_one))
    quarter_scratch = [
        pltpu.VMEM((2, quarter, 3 * channels), wide),
        pltpu.VMEM((2, quarter, channels), wide),
        sem((2, 2)),
    ]
    grad_shapes = [(qkv_weight.shape, wide), (proj_weight.shape, wide)]
    input_grad, qkv_grad, proj_grad = call_kernel(
        own_kernel,
        [((own_pixels, channels), low), *grad_shapes],
        quarter_scratch,
        [
            own_total,
            partial_sums,
            all_features,
            residual_grad,
            table,
            core_mixed,
            qkv_grad,
            proj_grad,
        ],
        "vvvvvvhh",
        conv_flops,
        12,
        "ohh",
        {6: 1, 7: 2},
    )
    input_grad, got_sums, chip_mixed, got_one, got_two = lax.optimization_barrier(
        (input_grad, got_sums, chip_mixed, got_one, got_two)
    )
    both_mixed = send_height(chip_mixed, 1)
    sums = sums + got_sums
    got_sums = send_canvas(sums, 2)
    qkv_grad, proj_grad = call_kernel(
        join_kernel,
        grad_shapes,
        quarter_scratch,
        [qkv_grad, proj_grad, chip_mixed, both_mixed],
        "hhvv",
        0,
        12,
        "hh",
        {0: 0, 1: 1},
    )
    qkv_grad, got_sums = lax.optimization_barrier((qkv_grad, got_sums))
    vector_shapes = [norm_gains.shape, norm_shifts.shape, conv_biases.shape, qv_bias.shape]
    conv_grad, gains_grad, shifts_grad, biases_grad, qv_grad, proj_bias_grad = call_kernel(
        sums_kernel,
        [((2, 3, 3, out_share, ci_share), wide)]
        + [(shape, wide) for shape in vector_shapes + [(1, channels)]],
        [],
        [sums, got_sums, hold_one, got_one, hold_two, got_two],
        "vvvvvv",
        0,
        12,
        "o" * 6,
    )
    own_shape = (1, local_rows, cols, channels)
    return (
        output.reshape(own_shape),
        input_grad.reshape(own_shape),
        gains_grad,
        shifts_grad,
        jnp.swapaxes(conv_grad, 3, 4),
        biases_grad,
        qkv_grad,
        qv_grad,
        proj_grad,
        proj_bias_grad.reshape(channels),
    )


def on_device(*arrays):
    features, tile_ids = arrays[0], arrays[1]
    local_rows, cols, channels = features.shape[1:]
    pixels = tile_ids.shape[1] * cols
    height_size, canvas_size = lax.axis_size("height"), lax.axis_size("canvas")
    powers = all(size & (size - 1) == 0 for size in (height_size, canvas_size, cols))
    fits = (
        powers
        and height_size > 2
        and canvas_size == 4
        and channels == LANES * canvas_size
        and pixels <= MOST_PIXELS
        and pixels % FILL_ROWS == 0
        and FILL_ROWS % CHUNK == 0
        and (local_rows * cols) % LANES == 0
        and CHUNK % cols == 0
        and cols % 16 == 0
        and channels % (LANES * canvas_size) == 0
        and 2 * channels == NARROW * height_size
    )
    return whole_canvas(*arrays) if fits else split_canvas(*arrays)


def solution(mesh):
    in_specs = (
        P("canvas", "height", None, None),
        P("canvas", None),
        P(),
        P(),
        P(),
        P(),
        P(),
        P(),
        P(),
        P(),
        P("canvas", "height", None, None),
    )
    out_specs = (
        P("canvas", "height", None, None),
        P("canvas", "height", None, None),
        P(),
        P(),
        P(None, None, None, "canvas", "height"),
        P(),
        P(),
        P(),
        P(),
        P(),
    )
    return jax.shard_map(
        on_device, mesh=mesh, in_specs=in_specs, out_specs=out_specs, check_vma=False
    )
```

```python
import functools

import jax
import jax.numpy as jnp
from jax import lax
from jax.experimental import pallas as pl
from jax.experimental.pallas import tpu as pltpu
from jax.sharding import PartitionSpec as P

GROUPS = 32


epsilon = 1e-06
masked_score = -1e30
MOST_PIXELS = 1024
LANES = 128
NARROW = 128
CHUNK = 128
FILL_ROWS = 256
QUERY_ROWS = 512


def extended(block, sides, width):
    for axis, dim in sides:
        count = lax.axis_size(axis)
        forward = [(i, i + 1) for i in range(count - 1)]
        backward = [(target, source) for source, target in forward]
        low = lax.ppermute(
            lax.slice_in_dim(block, block.shape[dim] - width, None, axis=dim), axis, forward
        )
        high = lax.ppermute(lax.slice_in_dim(block, 0, width, axis=dim), axis, backward)
        block = jnp.concatenate([low, block, high], axis=dim)
    return block


def group_total(vector):
    return vector.reshape(GROUPS, -1).sum(axis=1)


def spread_groups(vector, channels):
    return jnp.repeat(vector, channels // GROUPS)


def norm_forward(values, gain, shift, members):
    channels = values.shape[1]
    totals = lax.psum(group_total(jnp.sum(values, axis=0)), "height")
    centered = values - spread_groups(totals / members, channels)
    squares = lax.psum(group_total(jnp.sum(centered * centered, axis=0)), "height")
    inverse = spread_groups(lax.rsqrt(squares / members + epsilon), channels)
    normed = centered * inverse
    return (normed, inverse, normed * gain + shift)


def norm_backward(grad_in, normed, inverse, gain, members):
    channels = grad_in.shape[1]
    scaled = grad_in * gain
    both_sums = lax.psum(
        (group_total(jnp.sum(scaled, axis=0)), group_total(jnp.sum(scaled * normed, axis=0))),
        "height",
    )
    mean_grad = spread_groups(both_sums[0] / members, channels)
    mean_cross = spread_groups(both_sums[1] / members, channels)
    result = inverse * (scaled - mean_grad - normed * mean_cross)
    return (result, jnp.sum(grad_in * normed, axis=0), jnp.sum(grad_in, axis=0))


def swish(values):
    return values * jax.nn.sigmoid(values)


def swish_slope(values):
    sigmoid_part = jax.nn.sigmoid(values)
    return sigmoid_part * (1.0 + values * (1.0 - sigmoid_part))


def tap_columns(padded, row_mask, local_rows, canvas_cols):
    pieces = []
    for row_tap in range(3):
        rows_taken = padded[row_tap : row_tap + local_rows] * row_mask[:, row_tap, None, None]
        for col_tap in range(3):
            pieces.append(rows_taken[:, col_tap : col_tap + canvas_cols])
    stacked = jnp.concatenate(pieces, axis=2)
    return stacked.reshape(local_rows * canvas_cols, stacked.shape[2])


def conv_forward(acts, row_mask, weight, bias):
    local_rows, canvas_cols, channels = acts.shape
    rimmed = extended(acts, (("height", 0),), 1)
    padded = jnp.pad(rimmed, ((0, 0), (1, 1), (0, 0)))
    gathered = tap_columns(padded, row_mask, local_rows, canvas_cols)
    result = (
        jnp.dot(
            gathered, weight.reshape(9 * channels, channels), preferred_element_type=jnp.float32
        )
        + bias
    )
    return (result, gathered)


def conv_backward(grad_low, row_mask, weight, gathered):
    local_rows, canvas_cols, channels = grad_low.shape
    flat_grad = grad_low.reshape(local_rows * canvas_cols, channels)
    weight_grad = lax.dot_general(
        gathered, flat_grad, (((0,), (0,)), ((), ())), preferred_element_type=jnp.float32
    )
    rimmed = extended(grad_low, (("height", 0),), 1)
    padded = jnp.pad(rimmed, ((0, 0), (1, 1), (0, 0)))
    grad_taps = tap_columns(padded, row_mask, local_rows, canvas_cols)
    flipped = jnp.transpose(weight[::-1, ::-1], (0, 1, 3, 2)).reshape(9 * channels, channels)
    input_part = jnp.dot(grad_taps, flipped, preferred_element_type=jnp.float32)
    return (
        input_part,
        weight_grad.reshape(3, 3, channels, channels),
        jnp.sum(flat_grad.astype(jnp.float32), axis=0),
    )


def take_rows(array, offset, count):
    return lax.dynamic_slice_in_dim(array, offset, count)


def score_grads(
    queries, out_grad, log_total, row_dots, query_ids, key_rows, value_rows, key_ids, score_scale
):
    scores = (
        lax.dot_general(
            queries, key_rows, (((1,), (1,)), ((), ())), preferred_element_type=jnp.float32
        )
        * score_scale
    )
    same_tile = query_ids[:, None] == key_ids[None, :]
    softmax_block = jnp.exp(jnp.where(same_tile, scores - log_total[:, None], masked_score))
    weight_grad = lax.dot_general(
        out_grad, value_rows, (((1,), (1,)), ((), ())), preferred_element_type=jnp.float32
    )
    score_grad = (softmax_block * (weight_grad - row_dots[:, None])).astype(jnp.bfloat16)
    return (softmax_block.astype(jnp.bfloat16), score_grad)


def split_canvas(
    features,
    tile_ids,
    norm_gains,
    norm_shifts,
    conv_weights,
    conv_biases,
    qkv_weight,
    qv_bias,
    proj_weight,
    proj_bias,
    cotangent,
):
    height_size = lax.axis_size("height")
    local_rows = features.shape[1]
    canvas_cols = features.shape[2]
    channels = features.shape[3]
    pixels = local_rows * canvas_cols
    row_ids = tile_ids[0]
    all_rows = row_ids.shape[0]
    members = float(all_rows * canvas_cols * (channels // GROUPS))
    score_scale = channels ** (-0.5)
    first_row = lax.axis_index("height") * local_rows
    edge_ids = jnp.full((1,), -1, jnp.int32)
    padded_ids = jnp.concatenate([edge_ids, row_ids, edge_ids])
    near_ids = lax.dynamic_slice_in_dim(padded_ids, first_row, local_rows + 2)
    own_rows = near_ids[1 : local_rows + 1]
    row_mask = jnp.stack(
        [near_ids[row_tap : row_tap + local_rows] == own_rows for row_tap in range(3)], axis=1
    ).astype(jnp.bfloat16)
    key_ids = jnp.repeat(row_ids, canvas_cols)
    query_ids = jnp.repeat(own_rows, canvas_cols)
    grid_shape = (local_rows, canvas_cols, channels)
    inputs = features[0].reshape(pixels, channels).astype(jnp.float32)
    normed_one, inverse_one, pre_one = norm_forward(inputs, norm_gains[0], norm_shifts[0], members)
    act_one = swish(pre_one).astype(jnp.bfloat16).reshape(grid_shape)
    middle, taps_one = conv_forward(act_one, row_mask, conv_weights[0], conv_biases[0])
    normed_two, inverse_two, pre_two = norm_forward(middle, norm_gains[1], norm_shifts[1], members)
    act_two = swish(pre_two).astype(jnp.bfloat16).reshape(grid_shape)
    branch, taps_two = conv_forward(act_two, row_mask, conv_weights[1], conv_biases[1])
    residual = inputs + branch
    normed_three, inverse_three, pre_three = norm_forward(
        residual, norm_gains[2], norm_shifts[2], members
    )
    attn_input = pre_three.astype(jnp.bfloat16)
    mixed = jnp.dot(attn_input, qkv_weight, preferred_element_type=jnp.float32)
    queries = (mixed[:, :channels] + qv_bias[0]).astype(jnp.bfloat16)
    key_rows = mixed[:, channels : 2 * channels].astype(jnp.bfloat16)
    value_rows = (mixed[:, 2 * channels :] + qv_bias[1]).astype(jnp.bfloat16)
    running_max = jnp.full((pixels,), masked_score, jnp.float32)
    key_piece = lax.all_gather(key_rows, "height", axis=0, tiled=True)
    value_piece = lax.all_gather(value_rows, "height", axis=0, tiled=True)
    scores = (
        lax.dot_general(
            queries, key_piece, (((1,), (1,)), ((), ())), preferred_element_type=jnp.float32
        )
        * score_scale
    )
    same_tile = query_ids[:, None] == key_ids[None, :]
    scores = jnp.where(same_tile, scores, masked_score)
    new_max = jnp.maximum(running_max, jnp.max(scores, axis=1))
    weights = jnp.where(same_tile, jnp.exp(scores - new_max[:, None]), 0.0)
    summed_out = jnp.dot(
        weights.astype(jnp.bfloat16), value_piece, preferred_element_type=jnp.float32
    )
    total_weight = jnp.sum(weights, axis=1)
    log_total = new_max + jnp.log(total_weight)
    attended = summed_out / total_weight[:, None]
    attended_low = attended.astype(jnp.bfloat16)
    output = (
        residual
        + jnp.dot(attended_low, proj_weight, preferred_element_type=jnp.float32)
        + proj_bias
    )
    out_grad = cotangent[0].reshape(pixels, channels)
    out_grad_full = out_grad.astype(jnp.float32)
    proj_grad = lax.dot_general(
        attended_low, out_grad, (((0,), (0,)), ((), ())), preferred_element_type=jnp.float32
    )
    proj_bias_grad = jnp.sum(out_grad_full, axis=0)
    attended_grad = lax.dot_general(
        out_grad, proj_weight, (((1,), (1,)), ((), ())), preferred_element_type=jnp.float32
    ).astype(jnp.bfloat16)
    row_dots = jnp.sum(attended_grad.astype(jnp.float32) * attended, axis=1)
    block_rows = pixels * min(height_size, 8)
    zero_block = jnp.zeros((pixels, channels), jnp.float32)
    key_all, value_all = (
        lax.all_gather(key_rows, "height", axis=0, tiled=True),
        lax.all_gather(value_rows, "height", axis=0, tiled=True),
    )
    query_all, grad_all = (
        lax.all_gather(queries, "height", axis=0, tiled=True),
        lax.all_gather(attended_grad, "height", axis=0, tiled=True),
    )
    total_all, dots_all = (
        lax.all_gather(log_total, "height", axis=0, tiled=True),
        lax.all_gather(row_dots, "height", axis=0, tiled=True),
    )

    def own_query_step(running, block_index):
        offset = block_index * block_rows
        key_part = take_rows(key_all, offset, block_rows)
        rounded, score_grad = score_grads(
            queries,
            attended_grad,
            log_total,
            row_dots,
            query_ids,
            key_part,
            take_rows(value_all, offset, block_rows),
            take_rows(key_ids, offset, block_rows),
            score_scale,
        )
        return (
            running
            + jnp.dot(score_grad, key_part, preferred_element_type=jnp.float32) * score_scale,
            None,
        )

    def own_key_step(running, block_index):
        offset = block_index * block_rows
        query_part = take_rows(query_all, offset, block_rows)
        grad_part = take_rows(grad_all, offset, block_rows)
        rounded, score_grad = score_grads(
            query_part,
            grad_part,
            take_rows(total_all, offset, block_rows),
            take_rows(dots_all, offset, block_rows),
            take_rows(key_ids, offset, block_rows),
            key_rows,
            value_rows,
            query_ids,
            score_scale,
        )
        key_part = (
            lax.dot_general(
                score_grad, query_part, (((0,), (0,)), ((), ())), preferred_element_type=jnp.float32
            )
            * score_scale
        )
        value_part = lax.dot_general(
            rounded, grad_part, (((0,), (0,)), ((), ())), preferred_element_type=jnp.float32
        )
        return ((running[0] + key_part, running[1] + value_part), None)

    block_count = key_all.shape[0] // block_rows
    query_grad, unused_one = lax.scan(own_query_step, zero_block, jnp.arange(block_count))
    (key_grad, value_grad), unused_two = lax.scan(
        own_key_step, (zero_block, zero_block), jnp.arange(block_count)
    )
    query_low = query_grad.astype(jnp.bfloat16)
    key_low = key_grad.astype(jnp.bfloat16)
    value_low = value_grad.astype(jnp.bfloat16)
    stacked_grad = jnp.concatenate([query_low, key_low, value_low], axis=1)
    qkv_grad = lax.dot_general(
        attn_input, stacked_grad, (((0,), (0,)), ((), ())), preferred_element_type=jnp.float32
    )
    qv_grad = jnp.stack(
        [
            jnp.sum(query_low.astype(jnp.float32), axis=0),
            jnp.sum(value_low.astype(jnp.float32), axis=0),
        ]
    )
    normed_grad = lax.dot_general(
        stacked_grad, qkv_weight, (((1,), (1,)), ((), ())), preferred_element_type=jnp.float32
    )
    back_three, gain_three, shift_three = norm_backward(
        normed_grad, normed_three, inverse_three, norm_gains[2], members
    )
    residual_grad = out_grad_full + back_three
    grad_two = residual_grad.astype(jnp.bfloat16).reshape(grid_shape)
    act_two_grad, weight_two_grad, bias_two_grad = conv_backward(
        grad_two, row_mask, conv_weights[1], taps_two
    )
    middle_grad, gain_two, shift_two = norm_backward(
        act_two_grad * swish_slope(pre_two), normed_two, inverse_two, norm_gains[1], members
    )
    grad_one = middle_grad.astype(jnp.bfloat16).reshape(grid_shape)
    act_one_grad, weight_one_grad, bias_one_grad = conv_backward(
        grad_one, row_mask, conv_weights[0], taps_one
    )
    input_back, gain_one, shift_one = norm_backward(
        act_one_grad * swish_slope(pre_one), normed_one, inverse_one, norm_gains[0], members
    )
    input_grad = residual_grad + input_back
    conv_grad = jnp.stack([weight_one_grad, weight_two_grad])
    conv_part = lax.psum_scatter(conv_grad, "height", scatter_dimension=4, tiled=True)
    conv_part = lax.psum_scatter(
        conv_part.astype(jnp.bfloat16), "canvas", scatter_dimension=3, tiled=True
    ).astype(jnp.float32)
    summed = lax.psum(
        (
            jnp.stack([gain_one, gain_two, gain_three]),
            jnp.stack([shift_one, shift_two, shift_three]),
            jnp.stack([bias_one_grad, bias_two_grad]),
            qkv_grad,
            qv_grad,
            proj_grad,
            proj_bias_grad,
        ),
        ("canvas", "height"),
    )
    return (
        output.astype(jnp.bfloat16).reshape((1,) + grid_shape),
        input_grad.astype(jnp.bfloat16).reshape((1,) + grid_shape),
        summed[0],
        summed[1],
        conv_part,
        summed[2],
        summed[3],
        summed[4],
        summed[5],
        summed[6],
    )


def fold(block):
    rows, width = block.shape
    return jnp.sum(block.reshape(rows // 8, 8, width), axis=0)


def group_lanes(block, group):
    lane = lax.broadcasted_iota(jnp.int32, block.shape, 1)
    width = block.shape[1]
    step = 1
    while step < group:
        above = pltpu.roll(block, step, 1)
        below = pltpu.roll(block, width - step, 1)
        block = block + jnp.where((lane & step) != 0, above, below)
        step *= 2
    return block


def group_mean(partial, members):
    spread = group_lanes(partial, partial.shape[1] // GROUPS)
    return jnp.sum(spread, axis=0, keepdims=True) * (1.0 / members)


def widen(block, width):
    return jnp.concatenate([block] * (width // block.shape[1]), axis=1)


def each_block(pixels, block, body, carry=0):
    def step(index, carry):
        return body(pl.ds(pl.multiple_of(index * block, block), block), carry)

    return lax.fori_loop(0, pixels // block, step, carry)


def each_chunk(pixels, body, carry):
    return each_block(pixels, CHUNK, body, carry)


def aligned(start, step):
    return start if isinstance(start, int) else pl.multiple_of(start, step)


class RunningStats:
    def __init__(self, channels):
        self.width = channels // GROUPS
        self.reference = None
        self.sums = self.squares = jnp.zeros((8, channels), jnp.float32)

    def add(self, block):
        if self.reference is None:
            self.reference = group_mean(block[0:8], 8.0 * self.width)
        offset = block - self.reference
        self.sums = self.sums + fold(offset)
        self.squares = self.squares + fold(offset * offset)

    def finish(self, pixels):
        both = group_lanes(jnp.concatenate([self.sums, self.squares], axis=0), self.width)
        share = 1.0 / (pixels * self.width)
        offset = column_total(both[0:8]) * share
        variance = column_total(both[8:16]) * share - offset * offset
        return self.reference + offset, lax.rsqrt(jnp.maximum(variance, 0.0) + epsilon)


def put_taps(taps_ref, block, rows, cols):
    count, channels = block.shape
    place = lax.broadcasted_iota(jnp.int32, block.shape, 0) & (cols - 1)
    left = jnp.where(place == 0, 0.0, pltpu.roll(block, 1, 0))
    right = jnp.where(place == cols - 1, 0.0, pltpu.roll(block, count - 1, 0))
    inner = pl.ds(aligned(rows.start + cols, cols), count)
    taps_ref[inner, 0:channels] = left.astype(jnp.bfloat16)
    taps_ref[inner, channels : 2 * channels] = block.astype(jnp.bfloat16)
    taps_ref[inner, 2 * channels :] = right.astype(jnp.bfloat16)


def clear_edges(taps_ref, cols):
    edge = jnp.zeros((cols, taps_ref.shape[1]), taps_ref.dtype)
    taps_ref[0:cols, :] = edge
    taps_ref[taps_ref.shape[0] - cols :, :] = edge


def begin_conv(taps_ref, product, total_ref, fill, first, cols):
    for start in range(0, total_ref.shape[0], FILL_ROWS):
        for inner in range(start, start + FILL_ROWS, CHUNK):
            fill(pl.ds(inner, CHUNK))
        rows = pl.ds(start, FILL_ROWS)
        total_ref[rows, :] = first(rows, product(taps_ref, pl.ds(start + cols, FILL_ROWS), 1))


def add_rows(taps_ref, product, mask_ref, total_ref, row_tap, last, cols, old_ref=None):
    pixels, channels = total_ref.shape
    old_ref = total_ref if old_ref is None else old_ref
    for start in range(0, pixels, FILL_ROWS):
        rows = slice(start, start + FILL_ROWS)
        part = product(taps_ref, pl.ds(start + row_tap * cols, FILL_ROWS), row_tap)
        mask = widen(mask_ref[row_tap // 2, rows, :], channels)
        total_ref[rows, :] = last(rows, old_ref[rows, :] + mask * part)


def run_conv(taps_ref, product, mask_ref, total_ref, fill, first, last, cols):
    begin_conv(taps_ref, product, total_ref, fill, first, cols)
    add_rows(taps_ref, product, mask_ref, total_ref, 0, lambda rows, value: value, cols)
    add_rows(taps_ref, product, mask_ref, total_ref, 2, last, cols)


def product_forward(weight_ref):
    channels = weight_ref.shape[-1]

    def product(taps_ref, shifted, row_tap):
        return jnp.dot(
            taps_ref[shifted, :],
            weight_ref[row_tap].reshape(3 * channels, channels),
            preferred_element_type=jnp.float32,
        )

    return product


def product_backward(weight_ref):
    def product(taps_ref, shifted, row_tap):
        return lax.dot_general(
            taps_ref[shifted, :],
            weight_ref[row_tap],
            (((1,), (1,)), ((), ())),
            preferred_element_type=jnp.float32,
        )

    return product


def activation(read, mean, inverse, gain, shift, act_ref, taps_ref, cols):
    scale, offset = 0.5 * inverse * gain, 0.5 * shift

    def fill(rows):
        half = (read(rows) - mean) * scale + offset
        act = half * (1.0 + jnp.tanh(half))
        act_ref[rows, :] = act.astype(jnp.bfloat16)
        put_taps(taps_ref, act, rows, cols)

    return fill


def back_means(sums, gain, pixels):
    channels = gain.shape[1]
    members = float(pixels * (channels // GROUPS))
    return group_mean(sums[0] * gain, members), group_mean(sums[1] * gain, members)


def column_total(partial):
    return jnp.sum(partial, axis=0, keepdims=True)


def weight_part(act_ref, grad_ref, lanes_ref, flip_ref, columns_ref, part_ref, cols):
    pixels, channels = act_ref.shape
    height = lax.axis_index("height")
    share = NARROW // 2
    block = pl.ds(pl.multiple_of((height // 2) * NARROW, NARROW), NARROW)
    flip_ref[...] = grad_ref[:, block].T
    own = pl.ds(pl.multiple_of((height % 2) * share, share), share)
    grad = flip_ref[own, :].astype(jnp.float32)
    column = lax.broadcasted_iota(jnp.int32, grad.shape, 1) & (cols - 1)
    for col_tap in range(3):
        shifted = grad
        if col_tap == 0:
            shifted = jnp.where(column == cols - 1, 0.0, pltpu.roll(grad, pixels - 1, 1))
        elif col_tap == 2:
            shifted = jnp.where(column == 0, 0.0, pltpu.roll(grad, 1, 1))
        for row_tap in range(3):
            tap = 3 * row_tap + col_tap
            place = slice(tap * share, (tap + 1) * share)
            if row_tap == 1:
                columns_ref[place, :] = shifted.astype(jnp.bfloat16)
                continue
            side, turn = (0, pixels - cols) if row_tap == 0 else (1, cols)
            masked = (shifted * lanes_ref[side : side + 1, :]).astype(jnp.bfloat16)
            columns_ref[place, :] = pltpu.roll(masked, turn, 1)
    part_ref[...] = jnp.dot(
        columns_ref[...], act_ref[...], preferred_element_type=jnp.float32
    ).astype(jnp.bfloat16)


def begin_back(grad_ref, weights_ref, mask_ref, taps_ref, total_ref, cols):
    clear_edges(taps_ref, cols)

    def fill(rows):
        put_taps(taps_ref, grad_ref[rows, :].astype(jnp.float32), rows, cols)

    product = product_backward(weights_ref)
    begin_conv(taps_ref, product, total_ref, fill, lambda rows, part: part, cols)
    add_rows(taps_ref, product, mask_ref, total_ref, 0, lambda rows, value: value, cols)


def finish_back(
    weights_ref, mask_ref, taps_ref, total_ref, read, table_ref, which, cols, old_ref=None
):
    mean, inverse, gain, shift = norm_rows(table_ref, which)
    scale, offset = 0.5 * inverse * gain, 0.5 * shift
    sums = []

    def slope(rows, value):
        centered = read(rows) - mean
        half = centered * scale + offset
        turn = jnp.tanh(half)
        double = value * ((1.0 + turn) * (1.0 + half * (1.0 - turn)))
        sums.append((fold(double), fold(double * centered)))
        return double

    add_rows(
        taps_ref, product_backward(weights_ref), mask_ref, total_ref, 2, slope, cols, old_ref
    )
    plain, cross = sum(pair[0] for pair in sums), sum(pair[1] for pair in sums)
    return 0.5 * plain, 0.5 * inverse * cross


def norm_back(total_ref, double, sums, read, table_ref, which, pixels):
    mean, inverse, gain, shift = norm_rows(table_ref, which)
    mean_grad, mean_cross = back_means(sums, gain, pixels)
    slope = inverse * gain * (0.5 if double else 1.0)
    level, tilt = inverse * mean_grad, inverse * inverse * mean_cross

    def back(rows, inner):
        return total_ref[inner, :] * slope - level - (read(rows) - mean) * tilt

    return back


def turn_kernel(
    grad_ref, mask_ref, weights_ref, middle_ref, table_ref, total_ref, sums_ref, taps_ref, *, cols
):
    begin_back(grad_ref, weights_ref.at[1], mask_ref, taps_ref, total_ref, cols)
    sums_ref[0:8, :], sums_ref[8:16, :] = finish_back(
        weights_ref.at[1],
        mask_ref,
        taps_ref,
        total_ref,
        lambda rows: middle_ref[rows, :],
        table_ref,
        1,
        cols,
    )


def norm_rows(table_ref, which):
    picks = (2 * which, 2 * which + 1, 6 + which, 9 + which)
    return tuple(table_ref[pick : pick + 1, :] for pick in picks)


def build_masks(ids_ref, mask_ref, lanes_ref, id_rows_ref, id_cols_ref, cols):
    rows = ids_ref.shape[1]
    for row in range(rows):
        here = ids_ref[0, row]
        place = slice(row * cols, (row + 1) * cols)
        id_rows_ref[place, :] = jnp.full((cols, LANES), here, jnp.int32)
        for side, other in ((0, row - 1), (1, row + 1)):
            same = jnp.float32(0.0)
            if 0 <= other < rows:
                same = jnp.where(ids_ref[0, other] == here, 1.0, 0.0).astype(jnp.float32)
            mask_ref[side, place, :] = jnp.full((cols, LANES), same, jnp.float32)
    lane = lax.broadcasted_iota(jnp.int32, (8, LANES), 1)
    each = LANES // cols
    for block in range(rows // each):
        ids = jnp.full((8, LANES), ids_ref[0, block * each], jnp.int32)
        for step in range(1, each):
            ids = jnp.where(lane >= step * cols, ids_ref[0, block * each + step], ids)
        id_cols_ref[:, block * LANES : (block + 1) * LANES] = ids
    ids = id_cols_ref[...].astype(jnp.float32)
    pixels = ids.shape[1]
    pixel = lax.broadcasted_iota(jnp.int32, ids.shape, 1)
    above = jnp.where(pixel < cols, -1.0, pltpu.roll(ids, cols, 1))
    below = jnp.where(pixel >= pixels - cols, -1.0, pltpu.roll(ids, pixels - cols, 1))
    lanes_ref[0:1, :] = jnp.where(above == ids, 1.0, 0.0)[0:1]
    lanes_ref[1:2, :] = jnp.where(below == ids, 1.0, 0.0)[0:1]


def place_pieces(pieces, whole_ref, sems):
    own_pixels = whole_ref.shape[0] // len(pieces)
    height = lax.axis_index("height")
    copies = []
    for place, piece in enumerate(pieces):
        start = pl.multiple_of((height ^ place) * own_pixels, own_pixels)
        rows = pl.ds(start, own_pixels)
        copies.append(pltpu.make_async_copy(piece, whole_ref.at[rows, :], sems.at[place]))
    return copies


def hold_kernel(
    ids_hbm,
    gains_hbm,
    shifts_hbm,
    biases_hbm,
    weights_hbm,
    qkv_hbm,
    proj_hbm,
    qv_bias_hbm,
    proj_bias_hbm,
    weights_ref,
    turned_ref,
    qkv_ref,
    proj_ref,
    table_ref,
    mask_ref,
    lanes_ref,
    id_rows_ref,
    id_cols_ref,
    ids_ref,
    gains_ref,
    shifts_ref,
    biases_ref,
    qv_bias_ref,
    proj_bias_ref,
    sems,
    *,
    cols,
):
    channels = weights_ref.shape[-1]
    small = [
        (ids_hbm, ids_ref),
        (gains_hbm, gains_ref),
        (shifts_hbm, shifts_ref),
        (biases_hbm, biases_ref),
        (qv_bias_hbm, qv_bias_ref),
        (proj_bias_hbm, proj_bias_ref),
    ]
    large = [(weights_hbm, weights_ref), (qkv_hbm, qkv_ref), (proj_hbm, proj_ref)]
    for which in range(2):
        for row_tap in range(3):
            for col_tap in range(3):
                place = slice(col_tap * channels, (col_tap + 1) * channels)
                large.append(
                    (
                        weights_hbm.at[which, 2 - row_tap, 2 - col_tap],
                        turned_ref.at[which, row_tap, :, place],
                    )
                )
    copies = [
        pltpu.make_async_copy(source, target, sems.at[index])
        for index, (source, target) in enumerate(small + large)
    ]
    for copy in copies:
        copy.start()
    for copy in copies[: len(small)]:
        copy.wait()
    build_masks(ids_ref, mask_ref, lanes_ref, id_rows_ref, id_cols_ref, cols)
    table_ref[6:9, :] = gains_ref[...]
    table_ref[9:12, :] = shifts_ref[...]
    table_ref[12:14, :] = biases_ref[...]
    table_ref[14:16, :] = qv_bias_ref[...]
    table_ref[16:17, :] = proj_bias_ref[...]
    for copy in copies[len(small) :]:
        copy.wait()


def conv_kernel(*refs, cols, count):
    pieces, refs = refs[:count], refs[count:]
    (
        weights_ref,
        params_ref,
        mask_ref,
        features_ref,
        act_one_ref,
        middle_ref,
        act_two_ref,
        residual_ref,
        table_ref,
        own_ref,
        taps_ref,
        sem,
    ) = refs
    pixels, channels = features_ref.shape
    wide = jnp.float32
    own_copy = pltpu.make_async_copy(pieces[0], own_ref, sem)
    own_copy.start()
    table_ref[...] = params_ref[...]
    clear_edges(taps_ref, cols)

    def read_input(rows):
        return features_ref[rows, :].astype(wide)

    def read_middle(rows):
        return middle_ref[rows, :]

    height = lax.axis_index("height")
    own_pixels = pixels // count
    seen = RunningStats(channels)
    for place in list(range(1, count)) + [0]:
        if place == 0:
            own_copy.wait()
        piece = (pieces[place] if place else own_ref)[...]
        start = pl.multiple_of((height ^ place) * own_pixels, own_pixels)
        features_ref[pl.ds(start, own_pixels), :] = piece
        seen.add(piece.astype(wide))
    table_ref[0:1, :], table_ref[1:2, :] = seen.finish(pixels)
    seen = RunningStats(channels)

    def keep(rows, value):
        seen.add(value)
        return value

    run_conv(
        taps_ref,
        product_forward(weights_ref.at[0]),
        mask_ref,
        middle_ref,
        activation(read_input, *norm_rows(table_ref, 0), act_one_ref, taps_ref, cols),
        lambda rows, part: part + table_ref[12:13, :],
        keep,
        cols,
    )
    table_ref[2:3, :], table_ref[3:4, :] = seen.finish(pixels)
    seen = RunningStats(channels)
    run_conv(
        taps_ref,
        product_forward(weights_ref.at[1]),
        mask_ref,
        residual_ref,
        activation(read_middle, *norm_rows(table_ref, 1), act_two_ref, taps_ref, cols),
        lambda rows, part: part + (read_input(rows) + table_ref[13:14, :]),
        keep,
        cols,
    )
    table_ref[4:5, :], table_ref[5:6, :] = seen.finish(pixels)


def score_kernel(
    qkv_ref,
    proj_ref,
    residual_ref,
    table_ref,
    id_rows_ref,
    id_cols_ref,
    normed_ref,
    query_ref,
    key_ref,
    value_ref,
    soft_ref,
    out_flip_ref,
    output_ref,
    value_flip_ref,
    *,
    score_scale,
):
    pixels, channels = residual_ref.shape
    own_pixels = output_ref.shape[0]
    wide = jnp.float32
    exponent = score_scale * 1.4426950408889634
    mean, inverse, gain, shift = norm_rows(table_ref, 2)
    scale = inverse * gain
    block = min(QUERY_ROWS, pixels)

    def project(rows, carry):
        normed = ((residual_ref[rows, :] - mean) * scale + shift).astype(jnp.bfloat16)
        normed_ref[rows, :] = normed
        query_ref[rows, :] = (
            jnp.dot(normed, qkv_ref[:, 0:channels], preferred_element_type=wide)
            + table_ref[14:15, :]
        ).astype(jnp.bfloat16)
        key_ref[rows, :] = jnp.dot(
            normed, qkv_ref[:, channels : 2 * channels], preferred_element_type=wide
        ).astype(jnp.bfloat16)
        values = (
            jnp.dot(normed, qkv_ref[:, 2 * channels :], preferred_element_type=wide)
            + table_ref[15:16, :]
        ).astype(jnp.bfloat16)
        value_ref[rows, :] = values
        value_flip_ref[:, rows] = values.T
        return carry

    each_block(pixels, block, project)

    def attend(rows, carry):
        scores = lax.dot_general(
            key_ref[...], query_ref[rows, :], (((1,), (1,)), ((), ())), preferred_element_type=wide
        )
        same = widen(id_rows_ref[...], block) == id_cols_ref[0:1, rows]
        scores = jnp.where(same, scores, masked_score)
        scores = jnp.exp2((scores - jnp.max(scores, axis=0, keepdims=True)) * exponent)
        weights = scores * (1.0 / jnp.sum(scores, axis=0, keepdims=True))
        soft_ref[:, rows] = weights.astype(jnp.bfloat16)
        return carry

    each_block(pixels, block, attend)

    def collect(rows, carry):
        out_flip_ref[rows, :] = jnp.dot(
            value_flip_ref[rows, :], soft_ref[...], preferred_element_type=wide
        ).astype(jnp.bfloat16)
        return carry

    each_block(channels, channels // 2, collect)
    height = lax.axis_index("height")
    own = pl.ds(pl.multiple_of(height * own_pixels, own_pixels), own_pixels)
    output_ref[...] = (
        residual_ref[own, :]
        + lax.dot_general(
            out_flip_ref[:, own],
            proj_ref[...],
            (((0,), (0,)), ((), ())),
            preferred_element_type=wide,
        )
        + table_ref[16:17, :]
    ).astype(jnp.bfloat16)


def own_quarter():
    height = lax.axis_index("height")
    return (height & 1) * 2 + ((height >> 1) & 1)


def send_order(source_ref, targets, axis, share):
    me = lax.axis_index("canvas")
    for step, target in enumerate(targets):
        place = pl.ds(pl.multiple_of((me ^ step) * share, share), share)
        target[...] = source_ref[place, :] if axis == 0 else source_ref[:, place]


def attention_kernel(
    proj_ref,
    normed_ref,
    query_ref,
    key_ref,
    value_ref,
    soft_ref,
    out_flip_ref,
    *refs,
    score_scale,
    count,
):
    pieces, (grad_ref, packed_ref, sums_ref), refs = (
        refs[:count],
        refs[count : count + 3],
        refs[count + 3 :],
    )
    *mixed_refs, mixed_ref, key_flip_ref, back_ref, score_grad_ref, flip_ref, sems = refs
    pixels, channels = normed_ref.shape
    block = min(QUERY_ROWS, pixels)
    wide = jnp.float32
    copies = place_pieces(pieces, grad_ref, sems)
    for copy in copies:
        copy.start()
    quarter = channels // 4
    own = pl.ds(pl.multiple_of(own_quarter() * quarter, quarter), quarter)
    flip_ref[...] = normed_ref[:, own].T
    key_flip_ref[...] = key_ref[...].T
    for copy in copies:
        copy.wait()

    for start in range(0, pixels, block):
        rows = slice(start, start + block)
        back_ref[rows, :] = lax.dot_general(
            grad_ref[rows, :], proj_ref[...], (((1,), (1,)), ((), ())), preferred_element_type=wide
        ).astype(jnp.bfloat16)
    for start in range(0, pixels, block):
        rows = slice(start, start + block)
        weights = soft_ref[:, rows].astype(wide)
        weight_grad = lax.dot_general(
            value_ref[...],
            back_ref[rows, :],
            (((1,), (1,)), ((), ())),
            preferred_element_type=wide,
        )
        dots = jnp.sum(weights * weight_grad, axis=0, keepdims=True)
        score_grad = (weights * (weight_grad - dots)).astype(jnp.bfloat16)
        score_grad_ref[:, rows] = score_grad
        query_grad = jnp.dot(key_flip_ref[...], score_grad, preferred_element_type=wide)
        packed_ref[rows, 0:channels] = (query_grad * score_scale).astype(jnp.bfloat16).T
        packed_ref[rows, 2 * channels :] = jnp.dot(
            soft_ref[rows, :], back_ref[...], preferred_element_type=wide
        ).astype(jnp.bfloat16)
    for start in range(0, pixels, block):
        rows = slice(start, start + block)
        packed_ref[rows, channels : 2 * channels] = (
            jnp.dot(score_grad_ref[rows, :], query_ref[...], preferred_element_type=wide)
            * score_scale
        ).astype(jnp.bfloat16)

    def pack(rows, carry):
        return (
            carry[0] + fold(packed_ref[rows, 0:channels].astype(wide)),
            carry[1] + fold(packed_ref[rows, 2 * channels :].astype(wide)),
            carry[2] + fold(grad_ref[rows, :].astype(wide)),
        )

    zeros = jnp.zeros((8, channels), wide)
    totals = zeros, zeros, zeros
    for start in range(0, pixels, CHUNK):
        totals = pack(pl.ds(start, CHUNK), totals)
    sums_ref[...] = jnp.zeros(sums_ref.shape, wide)
    for row, total in enumerate(totals):
        sums_ref[8 + row : 9 + row, :] = column_total(total)
    mixed_ref[:, 0 : 3 * channels] = jnp.dot(
        flip_ref[...], packed_ref[...], preferred_element_type=wide
    ).astype(jnp.bfloat16)
    mixed_ref[:, 3 * channels :] = jnp.dot(
        out_flip_ref[own, :], grad_ref[...], preferred_element_type=wide
    ).astype(jnp.bfloat16)
    send_order(mixed_ref, mixed_refs, 0, quarter // len(mixed_refs))


def third_kernel(
    qkv_ref,
    grad_ref,
    packed_ref,
    residual_ref,
    table_ref,
    act_two_ref,
    lanes_ref,
    old_sums_ref,
    residual_grad_ref,
    grad_two_ref,
    sums_ref,
    keep_ref,
    send_ref,
    total_ref,
    flip_ref,
    columns_ref,
    part_ref,
    *,
    cols,
):
    pixels, channels = residual_ref.shape
    block = FILL_ROWS
    wide = jnp.float32
    mean, inverse, gain, shift = norm_rows(table_ref, 2)
    zeros = jnp.zeros((8, channels), wide)

    sums = (zeros, zeros)
    for start in range(0, pixels, block):
        rows = pl.ds(start, block)
        normed_grad = lax.dot_general(
            packed_ref[rows, :], qkv_ref[...], (((1,), (1,)), ((), ())), preferred_element_type=wide
        )
        total_ref[rows, :] = normed_grad
        centered = residual_ref[rows, :] - mean
        sums = sums[0] + fold(normed_grad), sums[1] + fold(normed_grad * centered)
    sums = sums[0], sums[1] * inverse
    sums_ref[...] = old_sums_ref[...]
    sums_ref[5:6, :] = column_total(sums[1])
    sums_ref[6:7, :] = column_total(sums[0])
    back = norm_back(
        total_ref, False, sums, lambda rows: residual_ref[rows, :], table_ref, 2, pixels
    )

    def finish(rows, carry):
        total = grad_ref[rows, :].astype(wide) + back(rows, rows)
        residual_grad_ref[rows, :] = total
        low = total.astype(jnp.bfloat16)
        grad_two_ref[rows, :] = low
        return carry + fold(low.astype(wide))

    sums_ref[7:8, :] = column_total(each_chunk(pixels, finish, zeros))
    weight_part(act_two_ref, grad_two_ref, lanes_ref, flip_ref, columns_ref, part_ref, cols)
    keep_half(part_ref, 2, 1, keep_ref, send_ref)


def second_kernel(
    total_ref,
    partial_ref,
    middle_ref,
    table_ref,
    act_one_ref,
    lanes_ref,
    old_sums_ref,
    grad_one_ref,
    sums_ref,
    keep_ref,
    send_ref,
    flip_ref,
    columns_ref,
    part_ref,
    *,
    cols,
):
    pixels, channels = middle_ref.shape
    sums = partial_ref[0:8, :], partial_ref[8:16, :]
    back = norm_back(
        total_ref, True, sums, lambda rows: middle_ref[rows, :], table_ref, 1, pixels
    )
    sums_ref[...] = old_sums_ref[...]
    sums_ref[2:3, :] = column_total(sums[1])
    sums_ref[3:4, :] = column_total(sums[0])

    def finish(rows, carry):
        low = back(rows, rows).astype(jnp.bfloat16)
        grad_one_ref[rows, :] = low
        return carry + fold(low.astype(jnp.float32))

    zeros = jnp.zeros((8, channels), jnp.float32)
    sums_ref[4:5, :] = column_total(each_chunk(pixels, finish, zeros))
    weight_part(act_one_ref, grad_one_ref, lanes_ref, flip_ref, columns_ref, part_ref, cols)
    keep_half(part_ref, 1, 2, keep_ref, send_ref)


def keep_half(part_ref, near, far, keep_ref, send_ref):
    me = lax.axis_index("canvas")
    rows, width = part_ref.shape[0], keep_ref.shape[1]
    for target_ref, flip in ((keep_ref, 0), (send_ref, near)):
        for slot in range(2):
            owner = me ^ flip ^ (slot * far)
            place = pl.ds(pl.multiple_of(owner * width, width), width)
            target_ref[slot * rows : (slot + 1) * rows, :] = part_ref[:, place]


def first_kernel(
    grad_one_ref,
    features_ref,
    table_ref,
    mask_ref,
    old_sums_ref,
    weights_ref,
    own_packed_ref,
    core_packed_ref,
    own_ref,
    sums_ref,
    partial_ref,
    qkv_hbm,
    proj_hbm,
    total_ref,
    taps_ref,
    qkv_ref,
    proj_ref,
    sems,
    *,
    cols,
):
    copies = spread_quarters(
        [own_packed_ref, core_packed_ref], [0, 2], qkv_ref, proj_ref, qkv_hbm, proj_hbm, sems
    )

    def read(rows):
        return features_ref[rows, :].astype(jnp.float32)

    weights = weights_ref.at[0]
    begin_back(grad_one_ref, weights, mask_ref, taps_ref, total_ref, cols)
    sums = finish_back(weights, mask_ref, taps_ref, total_ref, read, table_ref, 0, cols)
    partial_ref[0:8, :], partial_ref[8:16, :] = sums
    sums_ref[...] = old_sums_ref[...]
    sums_ref[0:1, :] = column_total(sums[1])
    sums_ref[1:2, :] = column_total(sums[0])
    count = own_ref.shape[0]
    own = pl.ds(pl.multiple_of(lax.axis_index("height") * count, count), count)
    own_ref[...] = total_ref[own, :]
    for copy in copies:
        copy.wait()


def own_kernel(
    own_ref, partial_ref, features_ref, residual_grad_ref, table_ref, input_grad_ref
):
    def read(rows):
        return features_ref[rows, :].astype(jnp.float32)

    sums = partial_ref[0:8, :], partial_ref[8:16, :]
    pixels = features_ref.shape[0]
    back = norm_back(own_ref, True, sums, read, table_ref, 0, pixels)
    count = own_ref.shape[0]
    own = pl.ds(pl.multiple_of(lax.axis_index("height") * count, count), count)
    total = residual_grad_ref[own, :] + back(own, slice(0, count))
    input_grad_ref[...] = total.astype(jnp.bfloat16)


def place_kernel(*refs):
    joints, packed_ref = refs[:-1], refs[-1]
    share = packed_ref.shape[0] // len(joints)
    me = lax.axis_index("canvas")
    for step, joint in enumerate(joints):
        place = pl.ds(pl.multiple_of((me ^ step) * share, share), share)
        packed_ref[place, :] = joint[...]


def spread_quarters(packed, flips, qkv_ref, proj_ref, qkv_hbm, proj_hbm, sems):
    quarter = packed[0].shape[0]
    inner = qkv_ref.shape[2]
    copies = []
    for index, packed_ref in enumerate(packed):
        owner = own_quarter() ^ flips[index]
        rows = pl.ds(pl.multiple_of(owner * quarter, quarter), quarter)
        qkv_ref[index] = packed_ref[:, 0:inner].astype(jnp.float32)
        proj_ref[index] = packed_ref[:, inner:].astype(jnp.float32)
        for which, (held, target) in enumerate(((qkv_ref, qkv_hbm), (proj_ref, proj_hbm))):
            copy = pltpu.make_async_copy(held.at[index], target.at[rows, :], sems.at[index, which])
            copy.start()
            copies.append(copy)
    return copies


def join_kernel(old_qkv, old_proj, chip_ref, qkv_hbm, proj_hbm, qkv_ref, proj_ref, sems):
    copies = spread_quarters([chip_ref], [1], qkv_ref, proj_ref, qkv_hbm, proj_hbm, sems)
    for copy in copies:
        copy.wait()


def halve_kernel(
    keep_one_ref,
    got_one_ref,
    keep_two_ref,
    got_two_ref,
    sums_ref,
    hold_one_ref,
    send_one_ref,
    hold_two_ref,
    send_two_ref,
):
    for keep_ref, got_ref, hold_ref, send_ref in (
        (keep_one_ref, got_one_ref, hold_one_ref, send_one_ref),
        (keep_two_ref, got_two_ref, hold_two_ref, send_two_ref),
    ):
        total = keep_ref[...].astype(jnp.float32) + got_ref[...].astype(jnp.float32)
        rows = hold_ref.shape[0]
        hold_ref[...] = total[0:rows]
        send_ref[0:rows, :] = total[rows:].astype(jnp.bfloat16)
    left = sums_ref[...]
    count, width = left.shape
    for part in range(3):
        low = left.astype(jnp.bfloat16)
        left = left - low.astype(jnp.float32)
        for block in range(width // LANES):
            piece = low[:, block * LANES : (block + 1) * LANES]
            for send_ref in (send_one_ref, send_two_ref):
                send_ref[rows : rows + count, :] = piece
            rows += count


def unpack_sums(got_ref, rows, count, width):
    total = jnp.zeros((count, width), jnp.float32)
    for part in range(3):
        blocks = []
        for block in range(width // LANES):
            blocks.append(got_ref[rows : rows + count, :].astype(jnp.float32))
            rows += count
        total = total + jnp.concatenate(blocks, axis=1)
    return total


def sums_kernel(
    sums_ref,
    far_ref,
    hold_one_ref,
    got_one_ref,
    hold_two_ref,
    got_two_ref,
    both_ref,
    old_qkv,
    old_proj,
    share_ref,
    gains_ref,
    shifts_ref,
    conv_ref,
    qv_ref,
    bias_ref,
    qkv_hbm,
    proj_hbm,
    qkv_ref,
    proj_ref,
    sems,
):
    copies = spread_quarters([both_ref], [3], qkv_ref, proj_ref, qkv_hbm, proj_hbm, sems)
    rows = hold_one_ref.shape[0]
    for which, (hold_ref, got_ref) in enumerate(
        ((hold_one_ref, got_one_ref), (hold_two_ref, got_two_ref))
    ):
        total = hold_ref[...] + got_ref[0:rows, :].astype(jnp.float32)
        share_ref[which] = total.reshape(share_ref.shape[1:])
    total = sums_ref[...] + far_ref[...]
    for got_ref in (got_one_ref, got_two_ref):
        total = total + unpack_sums(got_ref, rows, *total.shape)
    for row, start in enumerate((0, 2, 5)):
        gains_ref[row : row + 1, :] = total[start : start + 1]
        shifts_ref[row : row + 1, :] = total[start + 1 : start + 2]
    conv_ref[0:1, :] = total[4:5]
    conv_ref[1:2, :] = total[7:8]
    qv_ref[...] = total[8:10]
    bias_ref[...] = total[10:11]
    for copy in copies:
        copy.wait()


def call_kernel(kernel, outputs, scratch, operands, places, flops, limit, out_places=None, aliases={}):
    out_places = out_places or "v" * len(outputs)
    spaces = {
        "v": pl.BlockSpec(memory_space=pltpu.VMEM),
        "s": pl.BlockSpec(memory_space=pltpu.SMEM),
        "h": pl.BlockSpec(memory_space=pl.ANY),
        "o": pl.BlockSpec(memory_space=pltpu.VMEM),
        "a": pl.BlockSpec(memory_space=pl.ANY),
    }
    moved = 8 * flops // LANES
    held = {"v": pltpu.VMEM, "h": pltpu.HBM, "o": jax.ShapeDtypeStruct}
    operands = [
        pltpu.with_memory_space_constraint(array, pltpu.HBM) if place == "h" else array
        for array, place in zip(operands, places)
    ]
    return pl.pallas_call(
        kernel,
        out_shape=[held[place](*output) for output, place in zip(outputs, out_places)],
        in_specs=[spaces[place] for place in places],
        out_specs=[spaces[place] for place in out_places],
        scratch_shapes=scratch,
        input_output_aliases=aliases,
        compiler_params=pltpu.CompilerParams(vmem_limit_bytes=limit * 2**20),
        cost_estimate=pl.CostEstimate(flops=flops, bytes_accessed=moved, transcendentals=0),
    )(*operands)


def send_height(block, step):
    size = lax.axis_size("height")
    return lax.ppermute(block, "height", [(i, i ^ step) for i in range(size)])


def with_cores(blocks):
    return [piece for block in blocks for piece in (block, send_height(block, 1))]


def send_canvas(block, step):
    size = lax.axis_size("canvas")
    return lax.ppermute(block, "canvas", [(i, i ^ step) for i in range(size)])


def trade_canvas(pieces):
    return [pieces[0]] + [send_canvas(piece, step) for step, piece in enumerate(pieces) if step]


def whole_canvas(
    features,
    tile_ids,
    norm_gains,
    norm_shifts,
    conv_weights,
    conv_biases,
    qkv_weight,
    qv_bias,
    proj_weight,
    proj_bias,
    cotangent,
):
    height_size = lax.axis_size("height")
    canvas_size = lax.axis_size("canvas")
    local_rows, cols, channels = features.shape[1:]
    all_rows = tile_ids.shape[1]
    pixels = all_rows * cols
    own_pixels = local_rows * cols
    out_share = channels // height_size
    ci_share = channels // canvas_size
    quarter = channels // 4
    row_share = quarter // canvas_size
    low, wide = jnp.bfloat16, jnp.float32

    own_features = features.reshape(own_pixels, channels)
    own_grad = cotangent.reshape(own_pixels, channels)
    steps = range(2, height_size, 2)
    held_features = [own_features] + [send_height(own_features, step) for step in steps]
    plane = ((pixels, channels), low)
    plane_wide = ((pixels, channels), wide)
    sums_shape = ((16, channels), wide)
    mixed_shapes = [((row_share, 4 * channels), low)] * canvas_size
    taps = pltpu.VMEM((pixels + 2 * cols, 3 * channels), low)
    held_wide = pltpu.VMEM((pixels, channels), wide)
    flipped = pltpu.VMEM((channels, pixels), low)
    narrow = pltpu.VMEM((NARROW, pixels), low)
    columns = pltpu.VMEM((9 * out_share, pixels), low)
    part_held = pltpu.VMEM((9 * out_share, channels), low)
    sem = pltpu.SemaphoreType.DMA
    conv_flops = 2 * 9 * pixels * channels * channels
    dot_flops = 2 * pixels * channels * channels
    score_flops = 2 * pixels * pixels * channels
    scale = channels ** (-0.5)

    (
        held_conv,
        turned,
        held_qkv,
        held_proj,
        params,
        mask,
        lane_mask,
        id_rows,
        id_cols,
    ) = call_kernel(
        functools.partial(hold_kernel, cols=cols),
        [
            (conv_weights.shape, low),
            ((2, 3, channels, 3 * channels), low),
            (qkv_weight.shape, low),
            (proj_weight.shape, low),
            ((24, channels), wide),
            ((2, pixels, LANES), wide),
            ((8, pixels), wide),
            ((pixels, LANES), jnp.int32),
            ((8, pixels), jnp.int32),
        ],
        [
            pltpu.SMEM(tile_ids.shape, jnp.int32),
            pltpu.VMEM(norm_gains.shape, wide),
            pltpu.VMEM(norm_shifts.shape, wide),
            pltpu.VMEM(conv_biases.shape, wide),
            pltpu.VMEM(qv_bias.shape, wide),
            pltpu.VMEM((1, channels), wide),
            sem((27,)),
        ],
        [
            tile_ids,
            norm_gains,
            norm_shifts,
            conv_biases,
            conv_weights,
            qkv_weight,
            proj_weight,
            qv_bias,
            proj_bias.reshape(1, channels),
        ],
        "h" * 9,
        conv_flops,
        8,
    )
    held_features[1:] = [
        lax.optimization_barrier((params, block))[1] for block in held_features[1:]
    ]
    pieces = with_cores(held_features)
    far_grad, *pieces[4::2] = lax.optimization_barrier((own_grad, *held_features[2:]))
    held_grads = [own_grad, send_height(own_grad, 2)]
    held_grads[1], pieces[2] = lax.optimization_barrier((held_grads[1], held_features[1]))
    held_grads += [send_height(far_grad, step) for step in steps[1:]]

    all_features, act_one, middle, act_two, residual, table = call_kernel(
        functools.partial(conv_kernel, cols=cols, count=height_size),
        [plane, plane, plane_wide, plane, plane_wide, ((24, channels), wide)],
        [pltpu.VMEM((own_pixels, channels), low), taps, sem],
        [*pieces, held_conv, params, mask],
        "h" + "v" * (height_size + 2),
        2 * conv_flops,
        16,
    )
    residual, *held_grads = lax.optimization_barrier((residual, *held_grads))
    grad_pieces = with_cores(held_grads)
    normed, query, key, value, soft, out_flip, output = call_kernel(
        functools.partial(score_kernel, score_scale=scale),
        [
            plane,
            plane,
            plane,
            plane,
            ((pixels, pixels), low),
            ((channels, pixels), low),
            ((own_pixels, channels), low),
        ],
        [
            flipped,
        ],
        [
            held_qkv,
            held_proj,
            residual,
            table,
            id_rows,
            id_cols,
        ],
        "vvvvvv",
        3 * dot_flops + 2 * score_flops,
        16,
        "v" * 6 + "o",
    )
    normed, *grad_pieces = lax.optimization_barrier((normed, *grad_pieces))
    all_grad, packed, sums, *mixed = call_kernel(
        functools.partial(attention_kernel, score_scale=scale, count=height_size),
        [plane, ((pixels, 3 * channels), low), sums_shape, *mixed_shapes],
        [
            pltpu.VMEM((quarter, 4 * channels), low),
            flipped,
            pltpu.VMEM((pixels, channels), low),
            pltpu.VMEM((pixels, pixels), low),
            pltpu.VMEM((quarter, pixels), low),
            sem((height_size,)),
        ],
        [held_proj, normed, query, key, value, soft, out_flip, *grad_pieces],
        "vvvvvvvh" + "a" * (height_size - 1),
        3 * dot_flops + 4 * score_flops,
        20,
    )
    mixed = trade_canvas(mixed)
    halves = [((18 * out_share, ci_share), low)] * 2
    residual_grad, grad_two, sums, keep_two, send_two = call_kernel(
        functools.partial(third_kernel, cols=cols),
        [plane_wide, plane, sums_shape, *halves],
        [held_wide, narrow, columns, part_held],
        [held_qkv, all_grad, packed, residual, table, act_two, lane_mask, sums],
        "vvvvvvvv",
        3 * dot_flops + conv_flops // height_size,
        16,
    )
    grad_two, *mixed = lax.optimization_barrier((grad_two, *mixed))
    mixed_sum = mixed[0].astype(wide)
    for piece in mixed[1:]:
        mixed_sum = mixed_sum + piece.astype(wide)
    joints = trade_canvas([mixed_sum.astype(low)] * canvas_size)
    act_two_grad, partial_sums = call_kernel(
        functools.partial(turn_kernel, cols=cols),
        [plane_wide, sums_shape],
        [taps],
        [grad_two, mask, turned, middle, table],
        "vvvvv",
        conv_flops,
        16,
    )
    act_two_grad, *joints = lax.optimization_barrier((act_two_grad, *joints))
    (own_mixed,) = call_kernel(
        place_kernel,
        [((quarter, 4 * channels), low)],
        [],
        joints,
        "v" * canvas_size,
        1,
        12,
    )
    own_mixed, send_two = lax.optimization_barrier((own_mixed, send_two))
    got_two = send_canvas(send_two, 2)
    chip_mixed = send_height(own_mixed, 2)
    core_mixed = send_height(own_mixed, 1)
    grad_one, sums, keep_one, send_one = call_kernel(
        functools.partial(second_kernel, cols=cols),
        [plane, sums_shape, *halves],
        [narrow, columns, part_held],
        [act_two_grad, partial_sums, middle, table, act_one, lane_mask, sums],
        "vvvvvvv",
        1,
        16,
    )
    got_one = send_canvas(send_one, 1)

    def quarter_scratch(count):
        return [
            pltpu.VMEM((count, quarter, 3 * channels), wide),
            pltpu.VMEM((count, quarter, channels), wide),
            sem((count, 2)),
        ]

    grad_shapes = [(qkv_weight.shape, wide), (proj_weight.shape, wide)]
    grad_one, core_mixed = lax.optimization_barrier((grad_one, core_mixed))
    own_total, sums, partial_sums, qkv_grad, proj_grad = call_kernel(
        functools.partial(first_kernel, cols=cols),
        [((own_pixels, channels), wide), sums_shape, sums_shape, *grad_shapes],
        [held_wide, taps, *quarter_scratch(2)],
        [grad_one, all_features, table, mask, sums, turned, own_mixed, core_mixed],
        "vvvvvvvv",
        1,
        20,
        "vvvhh",
    )
    sums, got_one, got_two = lax.optimization_barrier((sums, got_one, got_two))
    share_rows = 9 * out_share
    send_rows = share_rows + 3 * sums_shape[0][0] * channels // LANES
    hold_one, send_one, hold_two, send_two = call_kernel(
        halve_kernel,
        [((share_rows, ci_share), wide), ((send_rows, ci_share), low)] * 2,
        [],
        [keep_one, got_one, keep_two, got_two, sums],
        "vvvvv",
        1,
        12,
    )
    got_one = send_canvas(send_one, 2)
    got_two = send_canvas(send_two, 1)
    far_sums = send_canvas(sums, 3)
    own_total, hold_one = lax.optimization_barrier((own_total, hold_one))
    (input_grad,) = call_kernel(
        own_kernel,
        [((own_pixels, channels), low)],
        [],
        [own_total, partial_sums, all_features, residual_grad, table],
        "vvvvv",
        dot_flops // 4,
        12,
        "o",
    )
    input_grad, got_one, got_two, far_sums = lax.optimization_barrier(
        (input_grad, got_one, got_two, far_sums)
    )
    chip_mixed, hold_one = lax.optimization_barrier((chip_mixed, hold_one))
    both_mixed = send_height(chip_mixed, 1)
    qkv_grad, proj_grad = call_kernel(
        join_kernel,
        grad_shapes,
        quarter_scratch(1),
        [qkv_grad, proj_grad, chip_mixed],
        "hhv",
        1,
        12,
        "hh",
        {0: 0, 1: 1},
    )
    vector_shapes = [norm_gains.shape, norm_shifts.shape, conv_biases.shape, qv_bias.shape]
    conv_grad, gains_grad, shifts_grad, biases_grad, qv_grad, proj_bias_grad, qkv_grad, proj_grad = (
        call_kernel(
            sums_kernel,
            [((2, 3, 3, out_share, ci_share), wide)]
            + [(shape, wide) for shape in vector_shapes + [(1, channels)]]
            + grad_shapes,
            quarter_scratch(1),
            [
                sums,
                far_sums,
                hold_one,
                got_one,
                hold_two,
                got_two,
                both_mixed,
                qkv_grad,
                proj_grad,
            ],
            "vvvvvvvhh",
            1,
            12,
            "oooooohh",
            {7: 6, 8: 7},
        )
    )
    own_shape = (1, local_rows, cols, channels)
    return (
        output.reshape(own_shape),
        input_grad.reshape(own_shape),
        gains_grad,
        shifts_grad,
        jnp.swapaxes(conv_grad, 3, 4),
        biases_grad,
        qkv_grad,
        qv_grad,
        proj_grad,
        proj_bias_grad.reshape(channels),
    )


def on_device(*arrays):
    features, tile_ids = arrays[0], arrays[1]
    local_rows, cols, channels = features.shape[1:]
    pixels = tile_ids.shape[1] * cols
    height_size, canvas_size = lax.axis_size("height"), lax.axis_size("canvas")
    powers = all(size & (size - 1) == 0 for size in (height_size, canvas_size, cols))
    fits = (
        powers
        and height_size > 2
        and canvas_size == 4
        and channels == LANES * canvas_size
        and pixels <= MOST_PIXELS
        and pixels % FILL_ROWS == 0
        and FILL_ROWS % CHUNK == 0
        and (local_rows * cols) % LANES == 0
        and CHUNK % cols == 0
        and cols % 16 == 0
        and channels % (LANES * canvas_size) == 0
        and 2 * channels == NARROW * height_size
    )
    return whole_canvas(*arrays) if fits else split_canvas(*arrays)


def solution(mesh):
    in_specs = (
        P("canvas", "height", None, None),
        P("canvas", None),
        P(),
        P(),
        P(),
        P(),
        P(),
        P(),
        P(),
        P(),
        P("canvas", "height", None, None),
    )
    out_specs = (
        P("canvas", "height", None, None),
        P("canvas", "height", None, None),
        P(),
        P(),
        P(None, None, None, "canvas", "height"),
        P(),
        P(),
        P(),
        P(),
        P(),
    )
    return jax.shard_map(
        on_device, mesh=mesh, in_specs=in_specs, out_specs=out_specs, check_vma=False
    )
```

```python
import functools

import jax
import jax.numpy as jnp
from jax import lax
from jax.experimental import pallas as pl
from jax.experimental.pallas import tpu as pltpu
from jax.sharding import PartitionSpec as P

GROUPS = 32


epsilon = 1e-06
masked_score = -1e30
MOST_PIXELS = 1024
LANES = 128
NARROW = 128
CHUNK = 128
FILL_ROWS = 256
QUERY_ROWS = 512
SCORE_ROWS = 256
KEY_ROWS = 256


def extended(block, sides, width):
    for axis, dim in sides:
        count = lax.axis_size(axis)
        forward = [(i, i + 1) for i in range(count - 1)]
        backward = [(target, source) for source, target in forward]
        low = lax.ppermute(
            lax.slice_in_dim(block, block.shape[dim] - width, None, axis=dim), axis, forward
        )
        high = lax.ppermute(lax.slice_in_dim(block, 0, width, axis=dim), axis, backward)
        block = jnp.concatenate([low, block, high], axis=dim)
    return block


def group_total(vector):
    return vector.reshape(GROUPS, -1).sum(axis=1)


def spread_groups(vector, channels):
    return jnp.repeat(vector, channels // GROUPS)


def norm_forward(values, gain, shift, members):
    channels = values.shape[1]
    totals = lax.psum(group_total(jnp.sum(values, axis=0)), "height")
    centered = values - spread_groups(totals / members, channels)
    squares = lax.psum(group_total(jnp.sum(centered * centered, axis=0)), "height")
    inverse = spread_groups(lax.rsqrt(squares / members + epsilon), channels)
    normed = centered * inverse
    return (normed, inverse, normed * gain + shift)


def norm_backward(grad_in, normed, inverse, gain, members):
    channels = grad_in.shape[1]
    scaled = grad_in * gain
    both_sums = lax.psum(
        (group_total(jnp.sum(scaled, axis=0)), group_total(jnp.sum(scaled * normed, axis=0))),
        "height",
    )
    mean_grad = spread_groups(both_sums[0] / members, channels)
    mean_cross = spread_groups(both_sums[1] / members, channels)
    result = inverse * (scaled - mean_grad - normed * mean_cross)
    return (result, jnp.sum(grad_in * normed, axis=0), jnp.sum(grad_in, axis=0))


def swish(values):
    return values * jax.nn.sigmoid(values)


def swish_slope(values):
    sigmoid_part = jax.nn.sigmoid(values)
    return sigmoid_part * (1.0 + values * (1.0 - sigmoid_part))


def tap_columns(padded, row_mask, local_rows, canvas_cols):
    pieces = []
    for row_tap in range(3):
        rows_taken = padded[row_tap : row_tap + local_rows] * row_mask[:, row_tap, None, None]
        for col_tap in range(3):
            pieces.append(rows_taken[:, col_tap : col_tap + canvas_cols])
    stacked = jnp.concatenate(pieces, axis=2)
    return stacked.reshape(local_rows * canvas_cols, stacked.shape[2])


def conv_forward(acts, row_mask, weight, bias):
    local_rows, canvas_cols, channels = acts.shape
    rimmed = extended(acts, (("height", 0),), 1)
    padded = jnp.pad(rimmed, ((0, 0), (1, 1), (0, 0)))
    gathered = tap_columns(padded, row_mask, local_rows, canvas_cols)
    result = (
        jnp.dot(
            gathered, weight.reshape(9 * channels, channels), preferred_element_type=jnp.float32
        )
        + bias
    )
    return (result, gathered)


def conv_backward(grad_low, row_mask, weight, gathered):
    local_rows, canvas_cols, channels = grad_low.shape
    flat_grad = grad_low.reshape(local_rows * canvas_cols, channels)
    weight_grad = lax.dot_general(
        gathered, flat_grad, (((0,), (0,)), ((), ())), preferred_element_type=jnp.float32
    )
    rimmed = extended(grad_low, (("height", 0),), 1)
    padded = jnp.pad(rimmed, ((0, 0), (1, 1), (0, 0)))
    grad_taps = tap_columns(padded, row_mask, local_rows, canvas_cols)
    flipped = jnp.transpose(weight[::-1, ::-1], (0, 1, 3, 2)).reshape(9 * channels, channels)
    input_part = jnp.dot(grad_taps, flipped, preferred_element_type=jnp.float32)
    return (
        input_part,
        weight_grad.reshape(3, 3, channels, channels),
        jnp.sum(flat_grad.astype(jnp.float32), axis=0),
    )


def take_rows(array, offset, count):
    return lax.dynamic_slice_in_dim(array, offset, count)


def score_grads(
    queries, out_grad, log_total, row_dots, query_ids, key_rows, value_rows, key_ids, score_scale
):
    scores = (
        lax.dot_general(
            queries, key_rows, (((1,), (1,)), ((), ())), preferred_element_type=jnp.float32
        )
        * score_scale
    )
    same_tile = query_ids[:, None] == key_ids[None, :]
    softmax_block = jnp.exp(jnp.where(same_tile, scores - log_total[:, None], masked_score))
    weight_grad = lax.dot_general(
        out_grad, value_rows, (((1,), (1,)), ((), ())), preferred_element_type=jnp.float32
    )
    score_grad = (softmax_block * (weight_grad - row_dots[:, None])).astype(jnp.bfloat16)
    return (softmax_block.astype(jnp.bfloat16), score_grad)


def split_canvas(
    features,
    tile_ids,
    norm_gains,
    norm_shifts,
    conv_weights,
    conv_biases,
    qkv_weight,
    qv_bias,
    proj_weight,
    proj_bias,
    cotangent,
):
    height_size = lax.axis_size("height")
    local_rows = features.shape[1]
    canvas_cols = features.shape[2]
    channels = features.shape[3]
    pixels = local_rows * canvas_cols
    row_ids = tile_ids[0]
    all_rows = row_ids.shape[0]
    members = float(all_rows * canvas_cols * (channels // GROUPS))
    score_scale = channels ** (-0.5)
    first_row = lax.axis_index("height") * local_rows
    edge_ids = jnp.full((1,), -1, jnp.int32)
    padded_ids = jnp.concatenate([edge_ids, row_ids, edge_ids])
    near_ids = lax.dynamic_slice_in_dim(padded_ids, first_row, local_rows + 2)
    own_rows = near_ids[1 : local_rows + 1]
    row_mask = jnp.stack(
        [near_ids[row_tap : row_tap + local_rows] == own_rows for row_tap in range(3)], axis=1
    ).astype(jnp.bfloat16)
    key_ids = jnp.repeat(row_ids, canvas_cols)
    query_ids = jnp.repeat(own_rows, canvas_cols)
    grid_shape = (local_rows, canvas_cols, channels)
    inputs = features[0].reshape(pixels, channels).astype(jnp.float32)
    normed_one, inverse_one, pre_one = norm_forward(inputs, norm_gains[0], norm_shifts[0], members)
    act_one = swish(pre_one).astype(jnp.bfloat16).reshape(grid_shape)
    middle, taps_one = conv_forward(act_one, row_mask, conv_weights[0], conv_biases[0])
    normed_two, inverse_two, pre_two = norm_forward(middle, norm_gains[1], norm_shifts[1], members)
    act_two = swish(pre_two).astype(jnp.bfloat16).reshape(grid_shape)
    branch, taps_two = conv_forward(act_two, row_mask, conv_weights[1], conv_biases[1])
    residual = inputs + branch
    normed_three, inverse_three, pre_three = norm_forward(
        residual, norm_gains[2], norm_shifts[2], members
    )
    attn_input = pre_three.astype(jnp.bfloat16)
    mixed = jnp.dot(attn_input, qkv_weight, preferred_element_type=jnp.float32)
    queries = (mixed[:, :channels] + qv_bias[0]).astype(jnp.bfloat16)
    key_rows = mixed[:, channels : 2 * channels].astype(jnp.bfloat16)
    value_rows = (mixed[:, 2 * channels :] + qv_bias[1]).astype(jnp.bfloat16)
    running_max = jnp.full((pixels,), masked_score, jnp.float32)
    key_piece = lax.all_gather(key_rows, "height", axis=0, tiled=True)
    value_piece = lax.all_gather(value_rows, "height", axis=0, tiled=True)
    scores = (
        lax.dot_general(
            queries, key_piece, (((1,), (1,)), ((), ())), preferred_element_type=jnp.float32
        )
        * score_scale
    )
    same_tile = query_ids[:, None] == key_ids[None, :]
    scores = jnp.where(same_tile, scores, masked_score)
    new_max = jnp.maximum(running_max, jnp.max(scores, axis=1))
    weights = jnp.where(same_tile, jnp.exp(scores - new_max[:, None]), 0.0)
    summed_out = jnp.dot(
        weights.astype(jnp.bfloat16), value_piece, preferred_element_type=jnp.float32
    )
    total_weight = jnp.sum(weights, axis=1)
    log_total = new_max + jnp.log(total_weight)
    attended = summed_out / total_weight[:, None]
    attended_low = attended.astype(jnp.bfloat16)
    output = (
        residual
        + jnp.dot(attended_low, proj_weight, preferred_element_type=jnp.float32)
        + proj_bias
    )
    out_grad = cotangent[0].reshape(pixels, channels)
    out_grad_full = out_grad.astype(jnp.float32)
    proj_grad = lax.dot_general(
        attended_low, out_grad, (((0,), (0,)), ((), ())), preferred_element_type=jnp.float32
    )
    proj_bias_grad = jnp.sum(out_grad_full, axis=0)
    attended_grad = lax.dot_general(
        out_grad, proj_weight, (((1,), (1,)), ((), ())), preferred_element_type=jnp.float32
    ).astype(jnp.bfloat16)
    row_dots = jnp.sum(attended_grad.astype(jnp.float32) * attended, axis=1)
    block_rows = pixels * min(height_size, 8)
    zero_block = jnp.zeros((pixels, channels), jnp.float32)
    key_all, value_all = (
        lax.all_gather(key_rows, "height", axis=0, tiled=True),
        lax.all_gather(value_rows, "height", axis=0, tiled=True),
    )
    query_all, grad_all = (
        lax.all_gather(queries, "height", axis=0, tiled=True),
        lax.all_gather(attended_grad, "height", axis=0, tiled=True),
    )
    total_all, dots_all = (
        lax.all_gather(log_total, "height", axis=0, tiled=True),
        lax.all_gather(row_dots, "height", axis=0, tiled=True),
    )

    def own_query_step(running, block_index):
        offset = block_index * block_rows
        key_part = take_rows(key_all, offset, block_rows)
        rounded, score_grad = score_grads(
            queries,
            attended_grad,
            log_total,
            row_dots,
            query_ids,
            key_part,
            take_rows(value_all, offset, block_rows),
            take_rows(key_ids, offset, block_rows),
            score_scale,
        )
        return (
            running
            + jnp.dot(score_grad, key_part, preferred_element_type=jnp.float32) * score_scale,
            None,
        )

    def own_key_step(running, block_index):
        offset = block_index * block_rows
        query_part = take_rows(query_all, offset, block_rows)
        grad_part = take_rows(grad_all, offset, block_rows)
        rounded, score_grad = score_grads(
            query_part,
            grad_part,
            take_rows(total_all, offset, block_rows),
            take_rows(dots_all, offset, block_rows),
            take_rows(key_ids, offset, block_rows),
            key_rows,
            value_rows,
            query_ids,
            score_scale,
        )
        key_part = (
            lax.dot_general(
                score_grad, query_part, (((0,), (0,)), ((), ())), preferred_element_type=jnp.float32
            )
            * score_scale
        )
        value_part = lax.dot_general(
            rounded, grad_part, (((0,), (0,)), ((), ())), preferred_element_type=jnp.float32
        )
        return ((running[0] + key_part, running[1] + value_part), None)

    block_count = key_all.shape[0] // block_rows
    query_grad, unused_one = lax.scan(own_query_step, zero_block, jnp.arange(block_count))
    (key_grad, value_grad), unused_two = lax.scan(
        own_key_step, (zero_block, zero_block), jnp.arange(block_count)
    )
    query_low = query_grad.astype(jnp.bfloat16)
    key_low = key_grad.astype(jnp.bfloat16)
    value_low = value_grad.astype(jnp.bfloat16)
    stacked_grad = jnp.concatenate([query_low, key_low, value_low], axis=1)
    qkv_grad = lax.dot_general(
        attn_input, stacked_grad, (((0,), (0,)), ((), ())), preferred_element_type=jnp.float32
    )
    qv_grad = jnp.stack(
        [
            jnp.sum(query_low.astype(jnp.float32), axis=0),
            jnp.sum(value_low.astype(jnp.float32), axis=0),
        ]
    )
    normed_grad = lax.dot_general(
        stacked_grad, qkv_weight, (((1,), (1,)), ((), ())), preferred_element_type=jnp.float32
    )
    back_three, gain_three, shift_three = norm_backward(
        normed_grad, normed_three, inverse_three, norm_gains[2], members
    )
    residual_grad = out_grad_full + back_three
    grad_two = residual_grad.astype(jnp.bfloat16).reshape(grid_shape)
    act_two_grad, weight_two_grad, bias_two_grad = conv_backward(
        grad_two, row_mask, conv_weights[1], taps_two
    )
    middle_grad, gain_two, shift_two = norm_backward(
        act_two_grad * swish_slope(pre_two), normed_two, inverse_two, norm_gains[1], members
    )
    grad_one = middle_grad.astype(jnp.bfloat16).reshape(grid_shape)
    act_one_grad, weight_one_grad, bias_one_grad = conv_backward(
        grad_one, row_mask, conv_weights[0], taps_one
    )
    input_back, gain_one, shift_one = norm_backward(
        act_one_grad * swish_slope(pre_one), normed_one, inverse_one, norm_gains[0], members
    )
    input_grad = residual_grad + input_back
    conv_grad = jnp.stack([weight_one_grad, weight_two_grad])
    conv_part = lax.psum_scatter(conv_grad, "height", scatter_dimension=4, tiled=True)
    conv_part = lax.psum_scatter(
        conv_part.astype(jnp.bfloat16), "canvas", scatter_dimension=3, tiled=True
    ).astype(jnp.float32)
    summed = lax.psum(
        (
            jnp.stack([gain_one, gain_two, gain_three]),
            jnp.stack([shift_one, shift_two, shift_three]),
            jnp.stack([bias_one_grad, bias_two_grad]),
            qkv_grad,
            qv_grad,
            proj_grad,
            proj_bias_grad,
        ),
        ("canvas", "height"),
    )
    return (
        output.astype(jnp.bfloat16).reshape((1,) + grid_shape),
        input_grad.astype(jnp.bfloat16).reshape((1,) + grid_shape),
        summed[0],
        summed[1],
        conv_part,
        summed[2],
        summed[3],
        summed[4],
        summed[5],
        summed[6],
    )


def fold(block):
    rows, width = block.shape
    return jnp.sum(block.reshape(rows // 8, 8, width), axis=0)


def group_lanes(block, group):
    lane = lax.broadcasted_iota(jnp.int32, block.shape, 1)
    width = block.shape[1]
    step = 1
    while step < group:
        above = pltpu.roll(block, step, 1)
        below = pltpu.roll(block, width - step, 1)
        block = block + jnp.where((lane & step) != 0, above, below)
        step *= 2
    return block


def group_mean(partial, members):
    spread = group_lanes(partial, partial.shape[1] // GROUPS)
    return jnp.sum(spread, axis=0, keepdims=True) * (1.0 / members)


def widen(block, width):
    return jnp.concatenate([block] * (width // block.shape[1]), axis=1)


def each_block(pixels, block, body, carry=0):
    def step(index, carry):
        return body(pl.ds(pl.multiple_of(index * block, block), block), carry)

    return lax.fori_loop(0, pixels // block, step, carry)


def each_chunk(pixels, body, carry):
    return each_block(pixels, CHUNK, body, carry)


def aligned(start, step):
    return start if isinstance(start, int) else pl.multiple_of(start, step)


class RunningStats:
    def __init__(self, channels):
        self.width = channels // GROUPS
        self.reference = None
        self.sums = self.squares = jnp.zeros((8, channels), jnp.float32)

    def add(self, block):
        if self.reference is None:
            self.reference = group_mean(block[0:8], 8.0 * self.width)
        offset = block - self.reference
        self.sums = self.sums + fold(offset)
        self.squares = self.squares + fold(offset * offset)

    def finish(self, pixels):
        both = group_lanes(jnp.concatenate([self.sums, self.squares], axis=0), self.width)
        share = 1.0 / (pixels * self.width)
        offset = column_total(both[0:8]) * share
        variance = column_total(both[8:16]) * share - offset * offset
        return self.reference + offset, lax.rsqrt(jnp.maximum(variance, 0.0) + epsilon)


def put_taps(taps_ref, block, rows, cols):
    count, channels = block.shape
    place = lax.broadcasted_iota(jnp.int32, block.shape, 0) & (cols - 1)
    left = jnp.where(place == 0, 0.0, pltpu.roll(block, 1, 0))
    right = jnp.where(place == cols - 1, 0.0, pltpu.roll(block, count - 1, 0))
    inner = pl.ds(aligned(rows.start + cols, cols), count)
    taps_ref[inner, 0:channels] = left.astype(jnp.bfloat16)
    taps_ref[inner, channels : 2 * channels] = block.astype(jnp.bfloat16)
    taps_ref[inner, 2 * channels :] = right.astype(jnp.bfloat16)


def clear_edges(taps_ref, cols):
    edge = jnp.zeros((cols, taps_ref.shape[1]), taps_ref.dtype)
    taps_ref[0:cols, :] = edge
    taps_ref[taps_ref.shape[0] - cols :, :] = edge


def begin_conv(taps_ref, product, total_ref, fill, first, cols):
    for start in range(0, total_ref.shape[0], FILL_ROWS):
        for inner in range(start, start + FILL_ROWS, CHUNK):
            fill(pl.ds(inner, CHUNK))
        rows = pl.ds(start, FILL_ROWS)
        total_ref[rows, :] = first(rows, product(taps_ref, pl.ds(start + cols, FILL_ROWS), 1))


def add_rows(taps_ref, product, mask_ref, total_ref, row_tap, last, cols, old_ref=None):
    pixels, channels = total_ref.shape
    old_ref = total_ref if old_ref is None else old_ref
    for start in range(0, pixels, FILL_ROWS):
        rows = slice(start, start + FILL_ROWS)
        part = product(taps_ref, pl.ds(start + row_tap * cols, FILL_ROWS), row_tap)
        mask = widen(mask_ref[row_tap // 2, rows, :], channels)
        total_ref[rows, :] = last(rows, old_ref[rows, :] + mask * part)


def run_conv(taps_ref, product, mask_ref, total_ref, fill, first, last, cols):
    begin_conv(taps_ref, product, total_ref, fill, first, cols)
    add_rows(taps_ref, product, mask_ref, total_ref, 0, lambda rows, value: value, cols)
    add_rows(taps_ref, product, mask_ref, total_ref, 2, last, cols)


def product_forward(weight_ref):
    channels = weight_ref.shape[-1]

    def product(taps_ref, shifted, row_tap):
        return jnp.dot(
            taps_ref[shifted, :],
            weight_ref[row_tap].reshape(3 * channels, channels),
            preferred_element_type=jnp.float32,
        )

    return product


def product_backward(weight_ref):
    def product(taps_ref, shifted, row_tap):
        return lax.dot_general(
            taps_ref[shifted, :],
            weight_ref[row_tap],
            (((1,), (1,)), ((), ())),
            preferred_element_type=jnp.float32,
        )

    return product


def activation(read, mean, inverse, gain, shift, act_ref, taps_ref, cols):
    scale, offset = 0.5 * inverse * gain, 0.5 * shift

    def fill(rows):
        half = (read(rows) - mean) * scale + offset
        act = half * (1.0 + jnp.tanh(half))
        act_ref[rows, :] = act.astype(jnp.bfloat16)
        put_taps(taps_ref, act, rows, cols)

    return fill


def back_means(sums, gain, pixels):
    channels = gain.shape[1]
    members = float(pixels * (channels // GROUPS))
    return group_mean(sums[0] * gain, members), group_mean(sums[1] * gain, members)


def column_total(partial):
    return jnp.sum(partial, axis=0, keepdims=True)


def weight_part(act_ref, grad_ref, lanes_ref, flip_ref, columns_ref, part_ref, cols):
    pixels, channels = act_ref.shape
    height = lax.axis_index("height")
    share = NARROW // 2
    block = pl.ds(pl.multiple_of((height // 2) * NARROW, NARROW), NARROW)
    flip_ref[...] = grad_ref[:, block].T
    own = pl.ds(pl.multiple_of((height % 2) * share, share), share)
    grad = flip_ref[own, :].astype(jnp.float32)
    column = lax.broadcasted_iota(jnp.int32, grad.shape, 1) & (cols - 1)
    for col_tap in range(3):
        shifted = grad
        if col_tap == 0:
            shifted = jnp.where(column == cols - 1, 0.0, pltpu.roll(grad, pixels - 1, 1))
        elif col_tap == 2:
            shifted = jnp.where(column == 0, 0.0, pltpu.roll(grad, 1, 1))
        for row_tap in range(3):
            tap = 3 * row_tap + col_tap
            place = slice(tap * share, (tap + 1) * share)
            if row_tap == 1:
                columns_ref[place, :] = shifted.astype(jnp.bfloat16)
                continue
            side, turn = (0, pixels - cols) if row_tap == 0 else (1, cols)
            masked = (shifted * lanes_ref[side : side + 1, :]).astype(jnp.bfloat16)
            columns_ref[place, :] = pltpu.roll(masked, turn, 1)
    part_ref[...] = jnp.dot(
        columns_ref[...], act_ref[...], preferred_element_type=jnp.float32
    ).astype(jnp.bfloat16)


def begin_back(grad_ref, weights_ref, mask_ref, taps_ref, total_ref, cols, aside=None):
    clear_edges(taps_ref, cols)

    def fill(rows):
        put_taps(taps_ref, grad_ref[rows, :].astype(jnp.float32), rows, cols)

    product = product_backward(weights_ref)
    begin_conv(taps_ref, product, total_ref, fill, lambda rows, part: part, cols)
    if aside is not None:
        aside()
    add_rows(taps_ref, product, mask_ref, total_ref, 0, lambda rows, value: value, cols)


def finish_back(
    weights_ref, mask_ref, taps_ref, total_ref, read, table_ref, which, cols, old_ref=None
):
    mean, inverse, gain, shift = norm_rows(table_ref, which)
    scale, offset = 0.5 * inverse * gain, 0.5 * shift
    sums = []

    def slope(rows, value):
        centered = read(rows) - mean
        half = centered * scale + offset
        turn = jnp.tanh(half)
        double = value * ((1.0 + turn) * (1.0 + half * (1.0 - turn)))
        sums.append((fold(double), fold(double * centered)))
        return double

    add_rows(
        taps_ref, product_backward(weights_ref), mask_ref, total_ref, 2, slope, cols, old_ref
    )
    plain, cross = sum(pair[0] for pair in sums), sum(pair[1] for pair in sums)
    return 0.5 * plain, 0.5 * inverse * cross


def norm_back(total_ref, double, sums, read, table_ref, which, pixels):
    mean, inverse, gain, shift = norm_rows(table_ref, which)
    mean_grad, mean_cross = back_means(sums, gain, pixels)
    slope = inverse * gain * (0.5 if double else 1.0)
    level, tilt = inverse * mean_grad, inverse * inverse * mean_cross

    def back(rows, inner):
        return total_ref[inner, :] * slope - level - (read(rows) - mean) * tilt

    return back


def turn_kernel(
    grad_ref, mask_ref, weights_ref, middle_ref, table_ref, total_ref, sums_ref, taps_ref, *, cols
):
    begin_back(grad_ref, weights_ref.at[1], mask_ref, taps_ref, total_ref, cols)
    sums_ref[0:8, :], sums_ref[8:16, :] = finish_back(
        weights_ref.at[1],
        mask_ref,
        taps_ref,
        total_ref,
        lambda rows: middle_ref[rows, :],
        table_ref,
        1,
        cols,
    )


def norm_rows(table_ref, which):
    picks = (2 * which, 2 * which + 1, 6 + which, 9 + which)
    return tuple(table_ref[pick : pick + 1, :] for pick in picks)


def build_masks(ids_ref, mask_ref, lanes_ref, id_rows_ref, id_cols_ref, cols):
    rows = ids_ref.shape[1]
    for row in range(rows):
        here = ids_ref[0, row]
        place = slice(row * cols, (row + 1) * cols)
        id_rows_ref[place, :] = jnp.full((cols, LANES), here, jnp.int32)
        for side, other in ((0, row - 1), (1, row + 1)):
            same = jnp.float32(0.0)
            if 0 <= other < rows:
                same = jnp.where(ids_ref[0, other] == here, 1.0, 0.0).astype(jnp.float32)
            mask_ref[side, place, :] = jnp.full((cols, LANES), same, jnp.float32)
    lane = lax.broadcasted_iota(jnp.int32, (8, LANES), 1)
    each = LANES // cols
    for block in range(rows // each):
        ids = jnp.full((8, LANES), ids_ref[0, block * each], jnp.int32)
        for step in range(1, each):
            ids = jnp.where(lane >= step * cols, ids_ref[0, block * each + step], ids)
        id_cols_ref[:, block * LANES : (block + 1) * LANES] = ids
    ids = id_cols_ref[...].astype(jnp.float32)
    pixels = ids.shape[1]
    pixel = lax.broadcasted_iota(jnp.int32, ids.shape, 1)
    above = jnp.where(pixel < cols, -1.0, pltpu.roll(ids, cols, 1))
    below = jnp.where(pixel >= pixels - cols, -1.0, pltpu.roll(ids, pixels - cols, 1))
    lanes_ref[0:1, :] = jnp.where(above == ids, 1.0, 0.0)[0:1]
    lanes_ref[1:2, :] = jnp.where(below == ids, 1.0, 0.0)[0:1]


def place_pieces(pieces, whole_ref, sems):
    own_pixels = whole_ref.shape[0] // len(pieces)
    height = lax.axis_index("height")
    copies = []
    for place, piece in enumerate(pieces):
        start = pl.multiple_of((height ^ place) * own_pixels, own_pixels)
        rows = pl.ds(start, own_pixels)
        copies.append(pltpu.make_async_copy(piece, whole_ref.at[rows, :], sems.at[place]))
    return copies


def hold_kernel(
    ids_hbm,
    gains_hbm,
    shifts_hbm,
    biases_hbm,
    weights_hbm,
    qkv_hbm,
    proj_hbm,
    qv_bias_hbm,
    proj_bias_hbm,
    weights_ref,
    turned_ref,
    qkv_ref,
    proj_ref,
    table_ref,
    mask_ref,
    lanes_ref,
    id_rows_ref,
    id_cols_ref,
    ids_ref,
    gains_ref,
    shifts_ref,
    biases_ref,
    qv_bias_ref,
    proj_bias_ref,
    sems,
    *,
    cols,
):
    channels = weights_ref.shape[-1]
    small = [
        (ids_hbm, ids_ref),
        (gains_hbm, gains_ref),
        (shifts_hbm, shifts_ref),
        (biases_hbm, biases_ref),
        (qv_bias_hbm, qv_bias_ref),
        (proj_bias_hbm, proj_bias_ref),
    ]
    large = [(weights_hbm, weights_ref), (qkv_hbm, qkv_ref), (proj_hbm, proj_ref)]
    for which in range(2):
        for row_tap in range(3):
            for col_tap in range(3):
                place = slice(col_tap * channels, (col_tap + 1) * channels)
                large.append(
                    (
                        weights_hbm.at[which, 2 - row_tap, 2 - col_tap],
                        turned_ref.at[which, row_tap, :, place],
                    )
                )
    copies = [
        pltpu.make_async_copy(source, target, sems.at[index])
        for index, (source, target) in enumerate(small + large)
    ]
    for copy in copies:
        copy.start()
    for copy in copies[: len(small)]:
        copy.wait()
    build_masks(ids_ref, mask_ref, lanes_ref, id_rows_ref, id_cols_ref, cols)
    table_ref[6:9, :] = gains_ref[...]
    table_ref[9:12, :] = shifts_ref[...]
    table_ref[12:14, :] = biases_ref[...]
    table_ref[14:16, :] = qv_bias_ref[...]
    table_ref[16:17, :] = proj_bias_ref[...]
    for copy in copies[len(small) :]:
        copy.wait()


def conv_kernel(*refs, cols, count):
    pieces, refs = refs[:count], refs[count:]
    (
        weights_ref,
        params_ref,
        mask_ref,
        features_ref,
        act_one_ref,
        middle_ref,
        act_two_ref,
        residual_ref,
        table_ref,
        own_ref,
        taps_ref,
        sem,
    ) = refs
    pixels, channels = features_ref.shape
    wide = jnp.float32
    own_copy = pltpu.make_async_copy(pieces[0], own_ref, sem)
    own_copy.start()
    table_ref[...] = params_ref[...]
    clear_edges(taps_ref, cols)

    def read_input(rows):
        return features_ref[rows, :].astype(wide)

    def read_middle(rows):
        return middle_ref[rows, :]

    height = lax.axis_index("height")
    own_pixels = pixels // count
    seen = RunningStats(channels)
    for place in list(range(1, count)) + [0]:
        if place == 0:
            own_copy.wait()
        piece = (pieces[place] if place else own_ref)[...]
        start = pl.multiple_of((height ^ place) * own_pixels, own_pixels)
        features_ref[pl.ds(start, own_pixels), :] = piece
        seen.add(piece.astype(wide))
    table_ref[0:1, :], table_ref[1:2, :] = seen.finish(pixels)
    seen = RunningStats(channels)

    def keep(rows, value):
        seen.add(value)
        return value

    run_conv(
        taps_ref,
        product_forward(weights_ref.at[0]),
        mask_ref,
        middle_ref,
        activation(read_input, *norm_rows(table_ref, 0), act_one_ref, taps_ref, cols),
        lambda rows, part: part + table_ref[12:13, :],
        keep,
        cols,
    )
    table_ref[2:3, :], table_ref[3:4, :] = seen.finish(pixels)
    seen = RunningStats(channels)
    run_conv(
        taps_ref,
        product_forward(weights_ref.at[1]),
        mask_ref,
        residual_ref,
        activation(read_middle, *norm_rows(table_ref, 1), act_two_ref, taps_ref, cols),
        lambda rows, part: part + (read_input(rows) + table_ref[13:14, :]),
        keep,
        cols,
    )
    table_ref[4:5, :], table_ref[5:6, :] = seen.finish(pixels)


def score_kernel(
    qkv_ref,
    proj_ref,
    residual_ref,
    table_ref,
    id_rows_ref,
    id_cols_ref,
    normed_ref,
    query_ref,
    key_ref,
    value_ref,
    soft_ref,
    out_flip_ref,
    output_ref,
    value_flip_ref,
    *scores_refs,
    score_scale,
):
    pixels, channels = residual_ref.shape
    own_pixels = output_ref.shape[0]
    wide = jnp.float32
    exponent = score_scale * 1.4426950408889634
    mean, inverse, gain, shift = norm_rows(table_ref, 2)
    scale = inverse * gain

    def project(rows, carry):
        normed = ((residual_ref[rows, :] - mean) * scale + shift).astype(jnp.bfloat16)
        normed_ref[rows, :] = normed
        query_ref[rows, :] = (
            jnp.dot(normed, qkv_ref[:, 0:channels], preferred_element_type=wide)
            + table_ref[14:15, :]
        ).astype(jnp.bfloat16)
        key_ref[rows, :] = jnp.dot(
            normed, qkv_ref[:, channels : 2 * channels], preferred_element_type=wide
        ).astype(jnp.bfloat16)
        values = (
            jnp.dot(normed, qkv_ref[:, 2 * channels :], preferred_element_type=wide)
            + table_ref[15:16, :]
        ).astype(jnp.bfloat16)
        value_ref[rows, :] = values
        value_flip_ref[:, rows] = values.T
        return carry

    each_block(pixels, min(QUERY_ROWS, pixels), project)
    block = scores_refs[0].shape[1]
    steps = range(0, pixels, KEY_ROWS)

    def score(index):
        rows = slice(index * block, (index + 1) * block)
        for start in steps:
            keys = slice(start, start + KEY_ROWS)
            scores = lax.dot_general(
                key_ref[keys, :],
                query_ref[rows, :],
                (((1,), (1,)), ((), ())),
                preferred_element_type=wide,
            )
            same = widen(id_rows_ref[keys, :], block) == id_cols_ref[0:1, rows]
            scores_refs[index][keys, :] = jnp.where(same, scores, masked_score)

    def soften(index):
        rows = slice(index * block, (index + 1) * block)
        scores_ref = scores_refs[index]
        peak = jnp.full((8, block), masked_score, wide)
        for start in steps:
            scores = scores_ref[start : start + KEY_ROWS, :]
            peak = jnp.maximum(peak, jnp.max(scores.reshape(-1, 8, block), axis=0))
        peak = jnp.max(peak, axis=0, keepdims=True)
        total = jnp.zeros((8, block), wide)
        for start in steps:
            keys = slice(start, start + KEY_ROWS)
            powers = jnp.exp2((scores_ref[keys, :] - peak) * exponent)
            scores_ref[keys, :] = powers
            total = total + fold(powers)
        share = 1.0 / column_total(total)
        for start in steps:
            keys = slice(start, start + KEY_ROWS)
            soft_ref[keys, rows] = (scores_ref[keys, :] * share).astype(jnp.bfloat16)

    score(0)
    for index in range(len(scores_refs)):
        if index + 1 < len(scores_refs):
            score(index + 1)
        soften(index)

    def collect(rows, carry):
        out_flip_ref[rows, :] = jnp.dot(
            value_flip_ref[rows, :], soft_ref[...], preferred_element_type=wide
        ).astype(jnp.bfloat16)
        return carry

    each_block(channels, channels // 2, collect)
    height = lax.axis_index("height")
    own = pl.ds(pl.multiple_of(height * own_pixels, own_pixels), own_pixels)
    output_ref[...] = (
        residual_ref[own, :]
        + lax.dot_general(
            out_flip_ref[:, own],
            proj_ref[...],
            (((0,), (0,)), ((), ())),
            preferred_element_type=wide,
        )
        + table_ref[16:17, :]
    ).astype(jnp.bfloat16)


def own_quarter():
    height = lax.axis_index("height")
    return (height & 1) * 2 + ((height >> 1) & 1)


def send_order(source_ref, targets, axis, share):
    me = lax.axis_index("canvas")
    for step, target in enumerate(targets):
        place = pl.ds(pl.multiple_of((me ^ step) * share, share), share)
        target[...] = source_ref[place, :] if axis == 0 else source_ref[:, place]


def attention_kernel(
    proj_ref,
    normed_ref,
    query_ref,
    key_ref,
    value_ref,
    soft_ref,
    out_flip_ref,
    *refs,
    score_scale,
    count,
):
    pieces, (grad_ref, packed_ref, sums_ref), refs = (
        refs[:count],
        refs[count : count + 3],
        refs[count + 3 :],
    )
    *mixed_refs, mixed_ref, key_flip_ref, back_ref, score_grad_ref, flip_ref, sems = refs
    pixels, channels = normed_ref.shape
    block = min(QUERY_ROWS, pixels)
    wide = jnp.float32
    copies = place_pieces(pieces, grad_ref, sems)
    for copy in copies:
        copy.start()
    quarter = channels // 4
    own = pl.ds(pl.multiple_of(own_quarter() * quarter, quarter), quarter)
    flip_ref[...] = normed_ref[:, own].T
    key_flip_ref[...] = key_ref[...].T
    for copy in copies:
        copy.wait()

    for start in range(0, pixels, block):
        rows = slice(start, start + block)
        back_ref[rows, :] = lax.dot_general(
            grad_ref[rows, :], proj_ref[...], (((1,), (1,)), ((), ())), preferred_element_type=wide
        ).astype(jnp.bfloat16)
    for start in range(0, pixels, block):
        rows = slice(start, start + block)
        weights = soft_ref[:, rows].astype(wide)
        weight_grad = lax.dot_general(
            value_ref[...],
            back_ref[rows, :],
            (((1,), (1,)), ((), ())),
            preferred_element_type=wide,
        )
        dots = jnp.sum(weights * weight_grad, axis=0, keepdims=True)
        score_grad = (weights * (weight_grad - dots)).astype(jnp.bfloat16)
        score_grad_ref[:, rows] = score_grad
        query_grad = jnp.dot(key_flip_ref[...], score_grad, preferred_element_type=wide)
        packed_ref[rows, 0:channels] = (query_grad * score_scale).astype(jnp.bfloat16).T
        packed_ref[rows, 2 * channels :] = jnp.dot(
            soft_ref[rows, :], back_ref[...], preferred_element_type=wide
        ).astype(jnp.bfloat16)
    for start in range(0, pixels, block):
        rows = slice(start, start + block)
        packed_ref[rows, channels : 2 * channels] = (
            jnp.dot(score_grad_ref[rows, :], query_ref[...], preferred_element_type=wide)
            * score_scale
        ).astype(jnp.bfloat16)

    def pack(rows, carry):
        return (
            carry[0] + fold(packed_ref[rows, 0:channels].astype(wide)),
            carry[1] + fold(packed_ref[rows, 2 * channels :].astype(wide)),
            carry[2] + fold(grad_ref[rows, :].astype(wide)),
        )

    zeros = jnp.zeros((8, channels), wide)
    totals = zeros, zeros, zeros
    for start in range(0, pixels, CHUNK):
        totals = pack(pl.ds(start, CHUNK), totals)
    sums_ref[...] = jnp.zeros(sums_ref.shape, wide)
    for row, total in enumerate(totals):
        sums_ref[8 + row : 9 + row, :] = column_total(total)
    mixed_ref[:, 0 : 3 * channels] = jnp.dot(
        flip_ref[...], packed_ref[...], preferred_element_type=wide
    ).astype(jnp.bfloat16)
    mixed_ref[:, 3 * channels :] = jnp.dot(
        out_flip_ref[own, :], grad_ref[...], preferred_element_type=wide
    ).astype(jnp.bfloat16)
    send_order(mixed_ref, mixed_refs, 0, quarter // len(mixed_refs))


def third_kernel(
    qkv_ref,
    grad_ref,
    packed_ref,
    residual_ref,
    table_ref,
    act_two_ref,
    lanes_ref,
    old_sums_ref,
    residual_grad_ref,
    grad_two_ref,
    sums_ref,
    keep_ref,
    send_ref,
    total_ref,
    flip_ref,
    columns_ref,
    part_ref,
    *,
    cols,
):
    pixels, channels = residual_ref.shape
    block = FILL_ROWS
    wide = jnp.float32
    mean, inverse, gain, shift = norm_rows(table_ref, 2)
    zeros = jnp.zeros((8, channels), wide)

    sums = (zeros, zeros)
    for start in range(0, pixels, block):
        rows = pl.ds(start, block)
        normed_grad = lax.dot_general(
            packed_ref[rows, :], qkv_ref[...], (((1,), (1,)), ((), ())), preferred_element_type=wide
        )
        total_ref[rows, :] = normed_grad
        centered = residual_ref[rows, :] - mean
        sums = sums[0] + fold(normed_grad), sums[1] + fold(normed_grad * centered)
    sums = sums[0], sums[1] * inverse
    sums_ref[...] = old_sums_ref[...]
    sums_ref[5:6, :] = column_total(sums[1])
    sums_ref[6:7, :] = column_total(sums[0])
    back = norm_back(
        total_ref, False, sums, lambda rows: residual_ref[rows, :], table_ref, 2, pixels
    )

    def finish(rows, carry):
        total = grad_ref[rows, :].astype(wide) + back(rows, rows)
        residual_grad_ref[rows, :] = total
        low = total.astype(jnp.bfloat16)
        grad_two_ref[rows, :] = low
        return carry + fold(low.astype(wide))

    sums_ref[7:8, :] = column_total(each_chunk(pixels, finish, zeros))
    weight_part(act_two_ref, grad_two_ref, lanes_ref, flip_ref, columns_ref, part_ref, cols)
    keep_half(part_ref, 2, 1, keep_ref, send_ref)


def second_kernel(
    total_ref,
    partial_ref,
    middle_ref,
    table_ref,
    act_one_ref,
    lanes_ref,
    old_sums_ref,
    grad_one_ref,
    sums_ref,
    keep_ref,
    send_ref,
    flip_ref,
    columns_ref,
    part_ref,
    *,
    cols,
):
    pixels, channels = middle_ref.shape
    sums = partial_ref[0:8, :], partial_ref[8:16, :]
    back = norm_back(
        total_ref, True, sums, lambda rows: middle_ref[rows, :], table_ref, 1, pixels
    )
    sums_ref[...] = old_sums_ref[...]
    sums_ref[2:3, :] = column_total(sums[1])
    sums_ref[3:4, :] = column_total(sums[0])

    def finish(rows, carry):
        low = back(rows, rows).astype(jnp.bfloat16)
        grad_one_ref[rows, :] = low
        return carry + fold(low.astype(jnp.float32))

    zeros = jnp.zeros((8, channels), jnp.float32)
    sums_ref[4:5, :] = column_total(each_chunk(pixels, finish, zeros))
    weight_part(act_one_ref, grad_one_ref, lanes_ref, flip_ref, columns_ref, part_ref, cols)
    keep_half(part_ref, 1, 2, keep_ref, send_ref)


def keep_half(part_ref, near, far, keep_ref, send_ref):
    me = lax.axis_index("canvas")
    rows, width = part_ref.shape[0], keep_ref.shape[1]
    for target_ref, flip in ((keep_ref, 0), (send_ref, near)):
        for slot in range(2):
            owner = me ^ flip ^ (slot * far)
            place = pl.ds(pl.multiple_of(owner * width, width), width)
            target_ref[slot * rows : (slot + 1) * rows, :] = part_ref[:, place]


def first_kernel(
    grad_one_ref,
    features_ref,
    table_ref,
    mask_ref,
    old_sums_ref,
    weights_ref,
    own_packed_ref,
    core_packed_ref,
    own_ref,
    sums_ref,
    partial_ref,
    qkv_hbm,
    proj_hbm,
    total_ref,
    taps_ref,
    qkv_ref,
    proj_ref,
    sems,
    *,
    cols,
):
    copies = []

    def read(rows):
        return features_ref[rows, :].astype(jnp.float32)

    def aside():
        packed = [own_packed_ref, core_packed_ref]
        copies.extend(
            spread_quarters(packed, [0, 2], qkv_ref, proj_ref, qkv_hbm, proj_hbm, sems)
        )

    weights = weights_ref.at[0]
    begin_back(grad_one_ref, weights, mask_ref, taps_ref, total_ref, cols, aside)
    sums = finish_back(weights, mask_ref, taps_ref, total_ref, read, table_ref, 0, cols)
    partial_ref[0:8, :], partial_ref[8:16, :] = sums
    sums_ref[...] = old_sums_ref[...]
    sums_ref[0:1, :] = column_total(sums[1])
    sums_ref[1:2, :] = column_total(sums[0])
    count = own_ref.shape[0]
    own = pl.ds(pl.multiple_of(lax.axis_index("height") * count, count), count)
    own_ref[...] = total_ref[own, :]
    for copy in copies:
        copy.wait()


def own_kernel(
    own_ref, partial_ref, features_ref, residual_grad_ref, table_ref, input_grad_ref
):
    def read(rows):
        return features_ref[rows, :].astype(jnp.float32)

    sums = partial_ref[0:8, :], partial_ref[8:16, :]
    pixels = features_ref.shape[0]
    back = norm_back(own_ref, True, sums, read, table_ref, 0, pixels)
    count = own_ref.shape[0]
    own = pl.ds(pl.multiple_of(lax.axis_index("height") * count, count), count)
    total = residual_grad_ref[own, :] + back(own, slice(0, count))
    input_grad_ref[...] = total.astype(jnp.bfloat16)


def place_kernel(*refs):
    joints, packed_ref = refs[:-1], refs[-1]
    share = packed_ref.shape[0] // len(joints)
    me = lax.axis_index("canvas")
    for step, joint in enumerate(joints):
        place = pl.ds(pl.multiple_of((me ^ step) * share, share), share)
        packed_ref[place, :] = joint[...]


def spread_quarters(packed, flips, qkv_ref, proj_ref, qkv_hbm, proj_hbm, sems):
    quarter = packed[0].shape[0]
    inner = qkv_ref.shape[2]
    copies = []
    for index, packed_ref in enumerate(packed):
        owner = own_quarter() ^ flips[index]
        rows = pl.ds(pl.multiple_of(owner * quarter, quarter), quarter)
        qkv_ref[index] = packed_ref[:, 0:inner].astype(jnp.float32)
        proj_ref[index] = packed_ref[:, inner:].astype(jnp.float32)
        for which, (held, target) in enumerate(((qkv_ref, qkv_hbm), (proj_ref, proj_hbm))):
            copy = pltpu.make_async_copy(held.at[index], target.at[rows, :], sems.at[index, which])
            copy.start()
            copies.append(copy)
    return copies


def join_kernel(
    old_qkv, old_proj, chip_ref, both_ref, qkv_hbm, proj_hbm, qkv_ref, proj_ref, sems
):
    copies = spread_quarters(
        [chip_ref, both_ref], [1, 3], qkv_ref, proj_ref, qkv_hbm, proj_hbm, sems
    )
    for copy in copies:
        copy.wait()


def halve_kernel(keep_ref, got_ref, hold_ref, send_ref):
    total = keep_ref[...].astype(jnp.float32) + got_ref[...].astype(jnp.float32)
    rows = hold_ref.shape[0]
    hold_ref[...] = total[0:rows]
    send_ref[0:rows, :] = total[rows:].astype(jnp.bfloat16)


def halve_sums_kernel(
    keep_one_ref,
    got_one_ref,
    keep_two_ref,
    got_two_ref,
    sums_ref,
    hold_ref,
    send_ref,
    hold_two_ref,
    send_two_ref,
):
    halve_kernel(keep_one_ref, got_one_ref, hold_ref, send_ref)
    halve_kernel(keep_two_ref, got_two_ref, hold_two_ref, send_two_ref)
    rows = hold_ref.shape[0]
    left = sums_ref[...]
    count, width = left.shape
    for part in range(2):
        low = left.astype(jnp.bfloat16)
        left = left - low.astype(jnp.float32)
        for block in range(width // LANES):
            send_ref[rows : rows + count, :] = low[:, block * LANES : (block + 1) * LANES]
            rows += count


def unpack_sums(got_ref, rows, count, width):
    total = jnp.zeros((count, width), jnp.float32)
    for part in range(2):
        blocks = []
        for block in range(width // LANES):
            blocks.append(got_ref[rows : rows + count, :].astype(jnp.float32))
            rows += count
        total = total + jnp.concatenate(blocks, axis=1)
    return total


def sums_kernel(
    sums_ref,
    near_ref,
    far_ref,
    hold_one_ref,
    got_one_ref,
    hold_two_ref,
    got_two_ref,
    share_ref,
    gains_ref,
    shifts_ref,
    conv_ref,
    qv_ref,
    bias_ref,
):
    rows = hold_one_ref.shape[0]
    for which, (hold_ref, got_ref) in enumerate(
        ((hold_one_ref, got_one_ref), (hold_two_ref, got_two_ref))
    ):
        total = hold_ref[...] + got_ref[0:rows, :].astype(jnp.float32)
        share_ref[which] = total.reshape(share_ref.shape[1:])
    total = sums_ref[...] + near_ref[...] + far_ref[...]
    total = total + unpack_sums(got_one_ref, rows, *total.shape)
    for row, start in enumerate((0, 2, 5)):
        gains_ref[row : row + 1, :] = total[start : start + 1]
        shifts_ref[row : row + 1, :] = total[start + 1 : start + 2]
    conv_ref[0:1, :] = total[4:5]
    conv_ref[1:2, :] = total[7:8]
    qv_ref[...] = total[8:10]
    bias_ref[...] = total[10:11]


def call_kernel(kernel, outputs, scratch, operands, places, flops, limit, out_places=None, aliases={}):
    out_places = out_places or "v" * len(outputs)
    spaces = {
        "v": pl.BlockSpec(memory_space=pltpu.VMEM),
        "s": pl.BlockSpec(memory_space=pltpu.SMEM),
        "h": pl.BlockSpec(memory_space=pl.ANY),
        "o": pl.BlockSpec(memory_space=pltpu.VMEM),
        "a": pl.BlockSpec(memory_space=pl.ANY),
    }
    moved = 8 * flops // LANES
    held = {"v": pltpu.VMEM, "h": pltpu.HBM, "o": jax.ShapeDtypeStruct}
    operands = [
        pltpu.with_memory_space_constraint(array, pltpu.HBM) if place == "h" else array
        for array, place in zip(operands, places)
    ]
    return pl.pallas_call(
        kernel,
        out_shape=[held[place](*output) for output, place in zip(outputs, out_places)],
        in_specs=[spaces[place] for place in places],
        out_specs=[spaces[place] for place in out_places],
        scratch_shapes=scratch,
        input_output_aliases=aliases,
        compiler_params=pltpu.CompilerParams(vmem_limit_bytes=limit * 2**20),
        cost_estimate=pl.CostEstimate(flops=flops, bytes_accessed=moved, transcendentals=0),
    )(*operands)


def send_height(block, step):
    size = lax.axis_size("height")
    return lax.ppermute(block, "height", [(i, i ^ step) for i in range(size)])


def with_cores(blocks):
    return [piece for block in blocks for piece in (block, send_height(block, 1))]


def send_canvas(block, step):
    size = lax.axis_size("canvas")
    return lax.ppermute(block, "canvas", [(i, i ^ step) for i in range(size)])


def trade_canvas(pieces):
    return [pieces[0]] + [send_canvas(piece, step) for step, piece in enumerate(pieces) if step]


def whole_canvas(
    features,
    tile_ids,
    norm_gains,
    norm_shifts,
    conv_weights,
    conv_biases,
    qkv_weight,
    qv_bias,
    proj_weight,
    proj_bias,
    cotangent,
):
    height_size = lax.axis_size("height")
    canvas_size = lax.axis_size("canvas")
    local_rows, cols, channels = features.shape[1:]
    all_rows = tile_ids.shape[1]
    pixels = all_rows * cols
    own_pixels = local_rows * cols
    out_share = channels // height_size
    ci_share = channels // canvas_size
    quarter = channels // 4
    row_share = quarter // canvas_size
    low, wide = jnp.bfloat16, jnp.float32

    own_features = features.reshape(own_pixels, channels)
    own_grad = cotangent.reshape(own_pixels, channels)
    steps = range(2, height_size, 2)
    held_features = [own_features] + [send_height(own_features, step) for step in steps]
    plane = ((pixels, channels), low)
    plane_wide = ((pixels, channels), wide)
    sums_shape = ((16, channels), wide)
    mixed_shapes = [((row_share, 4 * channels), low)] * canvas_size
    taps = pltpu.VMEM((pixels + 2 * cols, 3 * channels), low)
    held_wide = pltpu.VMEM((pixels, channels), wide)
    flipped = pltpu.VMEM((channels, pixels), low)
    narrow = pltpu.VMEM((NARROW, pixels), low)
    columns = pltpu.VMEM((9 * out_share, pixels), low)
    part_held = pltpu.VMEM((9 * out_share, channels), low)
    sem = pltpu.SemaphoreType.DMA
    conv_flops = 2 * 9 * pixels * channels * channels
    dot_flops = 2 * pixels * channels * channels
    score_flops = 2 * pixels * pixels * channels
    scale = channels ** (-0.5)

    (
        held_conv,
        turned,
        held_qkv,
        held_proj,
        params,
        mask,
        lane_mask,
        id_rows,
        id_cols,
    ) = call_kernel(
        functools.partial(hold_kernel, cols=cols),
        [
            (conv_weights.shape, low),
            ((2, 3, channels, 3 * channels), low),
            (qkv_weight.shape, low),
            (proj_weight.shape, low),
            ((24, channels), wide),
            ((2, pixels, LANES), wide),
            ((8, pixels), wide),
            ((pixels, LANES), jnp.int32),
            ((8, pixels), jnp.int32),
        ],
        [
            pltpu.SMEM(tile_ids.shape, jnp.int32),
            pltpu.VMEM(norm_gains.shape, wide),
            pltpu.VMEM(norm_shifts.shape, wide),
            pltpu.VMEM(conv_biases.shape, wide),
            pltpu.VMEM(qv_bias.shape, wide),
            pltpu.VMEM((1, channels), wide),
            sem((27,)),
        ],
        [
            tile_ids,
            norm_gains,
            norm_shifts,
            conv_biases,
            conv_weights,
            qkv_weight,
            proj_weight,
            qv_bias,
            proj_bias.reshape(1, channels),
        ],
        "h" * 9,
        conv_flops,
        8,
    )
    held_features[1:] = [
        lax.optimization_barrier((params, block))[1] for block in held_features[1:]
    ]
    pieces = with_cores(held_features)
    far_grad, *pieces[4::2] = lax.optimization_barrier((own_grad, *held_features[2:]))
    held_grads = [own_grad, send_height(own_grad, 2)]
    held_grads[1], pieces[2] = lax.optimization_barrier((held_grads[1], held_features[1]))
    held_grads += [send_height(far_grad, step) for step in steps[1:]]

    all_features, act_one, middle, act_two, residual, table = call_kernel(
        functools.partial(conv_kernel, cols=cols, count=height_size),
        [plane, plane, plane_wide, plane, plane_wide, ((24, channels), wide)],
        [pltpu.VMEM((own_pixels, channels), low), taps, sem],
        [*pieces, held_conv, params, mask],
        "h" + "v" * (height_size + 2),
        2 * conv_flops,
        16,
    )
    residual, *held_grads = lax.optimization_barrier((residual, *held_grads))
    grad_pieces = with_cores(held_grads)
    normed, query, key, value, soft, out_flip, output = call_kernel(
        functools.partial(score_kernel, score_scale=scale),
        [
            plane,
            plane,
            plane,
            plane,
            ((pixels, pixels), low),
            ((channels, pixels), low),
            ((own_pixels, channels), low),
        ],
        [
            flipped,
            *[pltpu.VMEM((pixels, SCORE_ROWS), wide)] * (pixels // SCORE_ROWS),
        ],
        [
            held_qkv,
            held_proj,
            residual,
            table,
            id_rows,
            id_cols,
        ],
        "vvvvvv",
        3 * dot_flops + 2 * score_flops,
        20,
        "v" * 6 + "o",
    )
    normed, *grad_pieces = lax.optimization_barrier((normed, *grad_pieces))
    all_grad, packed, sums, *mixed = call_kernel(
        functools.partial(attention_kernel, score_scale=scale, count=height_size),
        [plane, ((pixels, 3 * channels), low), sums_shape, *mixed_shapes],
        [
            pltpu.VMEM((quarter, 4 * channels), low),
            flipped,
            pltpu.VMEM((pixels, channels), low),
            pltpu.VMEM((pixels, pixels), low),
            pltpu.VMEM((quarter, pixels), low),
            sem((height_size,)),
        ],
        [held_proj, normed, query, key, value, soft, out_flip, *grad_pieces],
        "vvvvvvvh" + "a" * (height_size - 1),
        3 * dot_flops + 4 * score_flops,
        20,
    )
    mixed = trade_canvas(mixed)
    halves = [((18 * out_share, ci_share), low)] * 2
    residual_grad, grad_two, sums, keep_two, send_two = call_kernel(
        functools.partial(third_kernel, cols=cols),
        [plane_wide, plane, sums_shape, *halves],
        [held_wide, narrow, columns, part_held],
        [held_qkv, all_grad, packed, residual, table, act_two, lane_mask, sums],
        "vvvvvvvv",
        3 * dot_flops + conv_flops // height_size,
        16,
    )
    grad_two, *mixed = lax.optimization_barrier((grad_two, *mixed))
    mixed_sum = mixed[0].astype(wide)
    for piece in mixed[1:]:
        mixed_sum = mixed_sum + piece.astype(wide)
    joints = trade_canvas([mixed_sum.astype(low)] * canvas_size)
    act_two_grad, partial_sums = call_kernel(
        functools.partial(turn_kernel, cols=cols),
        [plane_wide, sums_shape],
        [taps],
        [grad_two, mask, turned, middle, table],
        "vvvvv",
        conv_flops,
        16,
    )
    act_two_grad, *joints = lax.optimization_barrier((act_two_grad, *joints))
    (own_mixed,) = call_kernel(
        place_kernel,
        [((quarter, 4 * channels), low)],
        [],
        joints,
        "v" * canvas_size,
        1,
        12,
    )
    own_mixed, send_two = lax.optimization_barrier((own_mixed, send_two))
    got_two = send_canvas(send_two, 2)
    chip_mixed = send_height(own_mixed, 2)
    core_mixed = send_height(own_mixed, 1)
    grad_one, sums, keep_one, send_one = call_kernel(
        functools.partial(second_kernel, cols=cols),
        [plane, sums_shape, *halves],
        [narrow, columns, part_held],
        [act_two_grad, partial_sums, middle, table, act_one, lane_mask, sums],
        "vvvvvvv",
        1,
        16,
    )
    got_one = send_canvas(send_one, 1)

    def quarter_scratch(count):
        return [
            pltpu.VMEM((count, quarter, 3 * channels), wide),
            pltpu.VMEM((count, quarter, channels), wide),
            sem((count, 2)),
        ]

    grad_shapes = [(qkv_weight.shape, wide), (proj_weight.shape, wide)]
    grad_one, core_mixed = lax.optimization_barrier((grad_one, core_mixed))
    own_total, sums, partial_sums, qkv_grad, proj_grad = call_kernel(
        functools.partial(first_kernel, cols=cols),
        [((own_pixels, channels), wide), sums_shape, sums_shape, *grad_shapes],
        [held_wide, taps, *quarter_scratch(2)],
        [grad_one, all_features, table, mask, sums, turned, own_mixed, core_mixed],
        "vvvvvvvv",
        1,
        20,
        "vvvhh",
    )
    share_rows = 9 * out_share
    send_rows = share_rows + 2 * sums_shape[0][0] * channels // LANES
    sums, got_one, got_two = lax.optimization_barrier((sums, got_one, got_two))
    hold_one, send_one, hold_two, send_two = call_kernel(
        halve_sums_kernel,
        [
            ((share_rows, ci_share), wide),
            ((send_rows, ci_share), low),
            ((share_rows, ci_share), wide),
            ((share_rows, ci_share), low),
        ],
        [],
        [keep_one, got_one, keep_two, got_two, sums],
        "vvvvv",
        1,
        12,
    )
    got_two = send_canvas(send_two, 1)
    got_one = send_canvas(send_one, 2)
    near_sums, far_sums = send_canvas(sums, 1), send_canvas(sums, 3)
    chip_mixed, hold_one = lax.optimization_barrier((chip_mixed, hold_one))
    both_mixed = send_height(chip_mixed, 1)
    own_total, hold_one = lax.optimization_barrier((own_total, hold_one))
    (input_grad,) = call_kernel(
        own_kernel,
        [((own_pixels, channels), low)],
        [],
        [own_total, partial_sums, all_features, residual_grad, table],
        "vvvvv",
        dot_flops // 4,
        12,
        "o",
    )
    input_grad, both_mixed, got_two = lax.optimization_barrier((input_grad, both_mixed, got_two))
    qkv_grad, proj_grad = call_kernel(
        join_kernel,
        grad_shapes,
        quarter_scratch(2),
        [qkv_grad, proj_grad, chip_mixed, both_mixed],
        "hhvv",
        1,
        12,
        "hh",
        {0: 0, 1: 1},
    )
    qkv_grad, got_one, near_sums, far_sums = lax.optimization_barrier(
        (qkv_grad, got_one, near_sums, far_sums)
    )
    vector_shapes = [norm_gains.shape, norm_shifts.shape, conv_biases.shape, qv_bias.shape]
    conv_grad, gains_grad, shifts_grad, biases_grad, qv_grad, proj_bias_grad = call_kernel(
        sums_kernel,
        [((2, 3, 3, out_share, ci_share), wide)]
        + [(shape, wide) for shape in vector_shapes + [(1, channels)]],
        [],
        [sums, near_sums, far_sums, hold_one, got_one, hold_two, got_two],
        "vvvvvvv",
        1,
        12,
        "o" * 6,
    )
    own_shape = (1, local_rows, cols, channels)
    return (
        output.reshape(own_shape),
        input_grad.reshape(own_shape),
        gains_grad,
        shifts_grad,
        jnp.swapaxes(conv_grad, 3, 4),
        biases_grad,
        qkv_grad,
        qv_grad,
        proj_grad,
        proj_bias_grad.reshape(channels),
    )


def on_device(*arrays):
    features, tile_ids = arrays[0], arrays[1]
    local_rows, cols, channels = features.shape[1:]
    pixels = tile_ids.shape[1] * cols
    height_size, canvas_size = lax.axis_size("height"), lax.axis_size("canvas")
    powers = all(size & (size - 1) == 0 for size in (height_size, canvas_size, cols))
    fits = (
        powers
        and height_size > 2
        and canvas_size == 4
        and channels == LANES * canvas_size
        and pixels <= MOST_PIXELS
        and pixels % FILL_ROWS == 0
        and FILL_ROWS % CHUNK == 0
        and pixels % SCORE_ROWS == 0
        and pixels % KEY_ROWS == 0
        and (local_rows * cols) % LANES == 0
        and CHUNK % cols == 0
        and cols % 16 == 0
        and channels % (LANES * canvas_size) == 0
        and 2 * channels == NARROW * height_size
    )
    return whole_canvas(*arrays) if fits else split_canvas(*arrays)


def solution(mesh):
    in_specs = (
        P("canvas", "height", None, None),
        P("canvas", None),
        P(),
        P(),
        P(),
        P(),
        P(),
        P(),
        P(),
        P(),
        P("canvas", "height", None, None),
    )
    out_specs = (
        P("canvas", "height", None, None),
        P("canvas", "height", None, None),
        P(),
        P(),
        P(None, None, None, "canvas", "height"),
        P(),
        P(),
        P(),
        P(),
        P(),
    )
    return jax.shard_map(
        on_device, mesh=mesh, in_specs=in_specs, out_specs=out_specs, check_vma=False
    )
```

```python
import functools

import jax
import jax.numpy as jnp
from jax import lax
from jax.experimental import pallas as pl
from jax.experimental.pallas import tpu as pltpu
from jax.sharding import PartitionSpec as P

GROUPS = 32


epsilon = 1e-06
masked_score = -1e30
MOST_PIXELS = 1024
LANES = 128
NARROW = 128
CHUNK = 128
FILL_ROWS = 256
QUERY_ROWS = 512
SCORE_ROWS = 256
KEY_ROWS = 256


def extended(block, sides, width):
    for axis, dim in sides:
        count = lax.axis_size(axis)
        forward = [(i, i + 1) for i in range(count - 1)]
        backward = [(target, source) for source, target in forward]
        low = lax.ppermute(
            lax.slice_in_dim(block, block.shape[dim] - width, None, axis=dim), axis, forward
        )
        high = lax.ppermute(lax.slice_in_dim(block, 0, width, axis=dim), axis, backward)
        block = jnp.concatenate([low, block, high], axis=dim)
    return block


def group_total(vector):
    return vector.reshape(GROUPS, -1).sum(axis=1)


def spread_groups(vector, channels):
    return jnp.repeat(vector, channels // GROUPS)


def norm_forward(values, gain, shift, members):
    channels = values.shape[1]
    totals = lax.psum(group_total(jnp.sum(values, axis=0)), "height")
    centered = values - spread_groups(totals / members, channels)
    squares = lax.psum(group_total(jnp.sum(centered * centered, axis=0)), "height")
    inverse = spread_groups(lax.rsqrt(squares / members + epsilon), channels)
    normed = centered * inverse
    return (normed, inverse, normed * gain + shift)


def norm_backward(grad_in, normed, inverse, gain, members):
    channels = grad_in.shape[1]
    scaled = grad_in * gain
    both_sums = lax.psum(
        (group_total(jnp.sum(scaled, axis=0)), group_total(jnp.sum(scaled * normed, axis=0))),
        "height",
    )
    mean_grad = spread_groups(both_sums[0] / members, channels)
    mean_cross = spread_groups(both_sums[1] / members, channels)
    result = inverse * (scaled - mean_grad - normed * mean_cross)
    return (result, jnp.sum(grad_in * normed, axis=0), jnp.sum(grad_in, axis=0))


def swish(values):
    return values * jax.nn.sigmoid(values)


def swish_slope(values):
    sigmoid_part = jax.nn.sigmoid(values)
    return sigmoid_part * (1.0 + values * (1.0 - sigmoid_part))


def tap_columns(padded, row_mask, local_rows, canvas_cols):
    pieces = []
    for row_tap in range(3):
        rows_taken = padded[row_tap : row_tap + local_rows] * row_mask[:, row_tap, None, None]
        for col_tap in range(3):
            pieces.append(rows_taken[:, col_tap : col_tap + canvas_cols])
    stacked = jnp.concatenate(pieces, axis=2)
    return stacked.reshape(local_rows * canvas_cols, stacked.shape[2])


def conv_forward(acts, row_mask, weight, bias):
    local_rows, canvas_cols, channels = acts.shape
    rimmed = extended(acts, (("height", 0),), 1)
    padded = jnp.pad(rimmed, ((0, 0), (1, 1), (0, 0)))
    gathered = tap_columns(padded, row_mask, local_rows, canvas_cols)
    result = (
        jnp.dot(
            gathered, weight.reshape(9 * channels, channels), preferred_element_type=jnp.float32
        )
        + bias
    )
    return (result, gathered)


def conv_backward(grad_low, row_mask, weight, gathered):
    local_rows, canvas_cols, channels = grad_low.shape
    flat_grad = grad_low.reshape(local_rows * canvas_cols, channels)
    weight_grad = lax.dot_general(
        gathered, flat_grad, (((0,), (0,)), ((), ())), preferred_element_type=jnp.float32
    )
    rimmed = extended(grad_low, (("height", 0),), 1)
    padded = jnp.pad(rimmed, ((0, 0), (1, 1), (0, 0)))
    grad_taps = tap_columns(padded, row_mask, local_rows, canvas_cols)
    flipped = jnp.transpose(weight[::-1, ::-1], (0, 1, 3, 2)).reshape(9 * channels, channels)
    input_part = jnp.dot(grad_taps, flipped, preferred_element_type=jnp.float32)
    return (
        input_part,
        weight_grad.reshape(3, 3, channels, channels),
        jnp.sum(flat_grad.astype(jnp.float32), axis=0),
    )


def take_rows(array, offset, count):
    return lax.dynamic_slice_in_dim(array, offset, count)


def score_grads(
    queries, out_grad, log_total, row_dots, query_ids, key_rows, value_rows, key_ids, score_scale
):
    scores = (
        lax.dot_general(
            queries, key_rows, (((1,), (1,)), ((), ())), preferred_element_type=jnp.float32
        )
        * score_scale
    )
    same_tile = query_ids[:, None] == key_ids[None, :]
    softmax_block = jnp.exp(jnp.where(same_tile, scores - log_total[:, None], masked_score))
    weight_grad = lax.dot_general(
        out_grad, value_rows, (((1,), (1,)), ((), ())), preferred_element_type=jnp.float32
    )
    score_grad = (softmax_block * (weight_grad - row_dots[:, None])).astype(jnp.bfloat16)
    return (softmax_block.astype(jnp.bfloat16), score_grad)


def split_canvas(
    features,
    tile_ids,
    norm_gains,
    norm_shifts,
    conv_weights,
    conv_biases,
    qkv_weight,
    qv_bias,
    proj_weight,
    proj_bias,
    cotangent,
):
    height_size = lax.axis_size("height")
    local_rows = features.shape[1]
    canvas_cols = features.shape[2]
    channels = features.shape[3]
    pixels = local_rows * canvas_cols
    row_ids = tile_ids[0]
    all_rows = row_ids.shape[0]
    members = float(all_rows * canvas_cols * (channels // GROUPS))
    score_scale = channels ** (-0.5)
    first_row = lax.axis_index("height") * local_rows
    edge_ids = jnp.full((1,), -1, jnp.int32)
    padded_ids = jnp.concatenate([edge_ids, row_ids, edge_ids])
    near_ids = lax.dynamic_slice_in_dim(padded_ids, first_row, local_rows + 2)
    own_rows = near_ids[1 : local_rows + 1]
    row_mask = jnp.stack(
        [near_ids[row_tap : row_tap + local_rows] == own_rows for row_tap in range(3)], axis=1
    ).astype(jnp.bfloat16)
    key_ids = jnp.repeat(row_ids, canvas_cols)
    query_ids = jnp.repeat(own_rows, canvas_cols)
    grid_shape = (local_rows, canvas_cols, channels)
    inputs = features[0].reshape(pixels, channels).astype(jnp.float32)
    normed_one, inverse_one, pre_one = norm_forward(inputs, norm_gains[0], norm_shifts[0], members)
    act_one = swish(pre_one).astype(jnp.bfloat16).reshape(grid_shape)
    middle, taps_one = conv_forward(act_one, row_mask, conv_weights[0], conv_biases[0])
    normed_two, inverse_two, pre_two = norm_forward(middle, norm_gains[1], norm_shifts[1], members)
    act_two = swish(pre_two).astype(jnp.bfloat16).reshape(grid_shape)
    branch, taps_two = conv_forward(act_two, row_mask, conv_weights[1], conv_biases[1])
    residual = inputs + branch
    normed_three, inverse_three, pre_three = norm_forward(
        residual, norm_gains[2], norm_shifts[2], members
    )
    attn_input = pre_three.astype(jnp.bfloat16)
    mixed = jnp.dot(attn_input, qkv_weight, preferred_element_type=jnp.float32)
    queries = (mixed[:, :channels] + qv_bias[0]).astype(jnp.bfloat16)
    key_rows = mixed[:, channels : 2 * channels].astype(jnp.bfloat16)
    value_rows = (mixed[:, 2 * channels :] + qv_bias[1]).astype(jnp.bfloat16)
    running_max = jnp.full((pixels,), masked_score, jnp.float32)
    key_piece = lax.all_gather(key_rows, "height", axis=0, tiled=True)
    value_piece = lax.all_gather(value_rows, "height", axis=0, tiled=True)
    scores = (
        lax.dot_general(
            queries, key_piece, (((1,), (1,)), ((), ())), preferred_element_type=jnp.float32
        )
        * score_scale
    )
    same_tile = query_ids[:, None] == key_ids[None, :]
    scores = jnp.where(same_tile, scores, masked_score)
    new_max = jnp.maximum(running_max, jnp.max(scores, axis=1))
    weights = jnp.where(same_tile, jnp.exp(scores - new_max[:, None]), 0.0)
    summed_out = jnp.dot(
        weights.astype(jnp.bfloat16), value_piece, preferred_element_type=jnp.float32
    )
    total_weight = jnp.sum(weights, axis=1)
    log_total = new_max + jnp.log(total_weight)
    attended = summed_out / total_weight[:, None]
    attended_low = attended.astype(jnp.bfloat16)
    output = (
        residual
        + jnp.dot(attended_low, proj_weight, preferred_element_type=jnp.float32)
        + proj_bias
    )
    out_grad = cotangent[0].reshape(pixels, channels)
    out_grad_full = out_grad.astype(jnp.float32)
    proj_grad = lax.dot_general(
        attended_low, out_grad, (((0,), (0,)), ((), ())), preferred_element_type=jnp.float32
    )
    proj_bias_grad = jnp.sum(out_grad_full, axis=0)
    attended_grad = lax.dot_general(
        out_grad, proj_weight, (((1,), (1,)), ((), ())), preferred_element_type=jnp.float32
    ).astype(jnp.bfloat16)
    row_dots = jnp.sum(attended_grad.astype(jnp.float32) * attended, axis=1)
    block_rows = pixels * min(height_size, 8)
    zero_block = jnp.zeros((pixels, channels), jnp.float32)
    key_all, value_all = (
        lax.all_gather(key_rows, "height", axis=0, tiled=True),
        lax.all_gather(value_rows, "height", axis=0, tiled=True),
    )
    query_all, grad_all = (
        lax.all_gather(queries, "height", axis=0, tiled=True),
        lax.all_gather(attended_grad, "height", axis=0, tiled=True),
    )
    total_all, dots_all = (
        lax.all_gather(log_total, "height", axis=0, tiled=True),
        lax.all_gather(row_dots, "height", axis=0, tiled=True),
    )

    def own_query_step(running, block_index):
        offset = block_index * block_rows
        key_part = take_rows(key_all, offset, block_rows)
        rounded, score_grad = score_grads(
            queries,
            attended_grad,
            log_total,
            row_dots,
            query_ids,
            key_part,
            take_rows(value_all, offset, block_rows),
            take_rows(key_ids, offset, block_rows),
            score_scale,
        )
        return (
            running
            + jnp.dot(score_grad, key_part, preferred_element_type=jnp.float32) * score_scale,
            None,
        )

    def own_key_step(running, block_index):
        offset = block_index * block_rows
        query_part = take_rows(query_all, offset, block_rows)
        grad_part = take_rows(grad_all, offset, block_rows)
        rounded, score_grad = score_grads(
            query_part,
            grad_part,
            take_rows(total_all, offset, block_rows),
            take_rows(dots_all, offset, block_rows),
            take_rows(key_ids, offset, block_rows),
            key_rows,
            value_rows,
            query_ids,
            score_scale,
        )
        key_part = (
            lax.dot_general(
                score_grad, query_part, (((0,), (0,)), ((), ())), preferred_element_type=jnp.float32
            )
            * score_scale
        )
        value_part = lax.dot_general(
            rounded, grad_part, (((0,), (0,)), ((), ())), preferred_element_type=jnp.float32
        )
        return ((running[0] + key_part, running[1] + value_part), None)

    block_count = key_all.shape[0] // block_rows
    query_grad, unused_one = lax.scan(own_query_step, zero_block, jnp.arange(block_count))
    (key_grad, value_grad), unused_two = lax.scan(
        own_key_step, (zero_block, zero_block), jnp.arange(block_count)
    )
    query_low = query_grad.astype(jnp.bfloat16)
    key_low = key_grad.astype(jnp.bfloat16)
    value_low = value_grad.astype(jnp.bfloat16)
    stacked_grad = jnp.concatenate([query_low, key_low, value_low], axis=1)
    qkv_grad = lax.dot_general(
        attn_input, stacked_grad, (((0,), (0,)), ((), ())), preferred_element_type=jnp.float32
    )
    qv_grad = jnp.stack(
        [
            jnp.sum(query_low.astype(jnp.float32), axis=0),
            jnp.sum(value_low.astype(jnp.float32), axis=0),
        ]
    )
    normed_grad = lax.dot_general(
        stacked_grad, qkv_weight, (((1,), (1,)), ((), ())), preferred_element_type=jnp.float32
    )
    back_three, gain_three, shift_three = norm_backward(
        normed_grad, normed_three, inverse_three, norm_gains[2], members
    )
    residual_grad = out_grad_full + back_three
    grad_two = residual_grad.astype(jnp.bfloat16).reshape(grid_shape)
    act_two_grad, weight_two_grad, bias_two_grad = conv_backward(
        grad_two, row_mask, conv_weights[1], taps_two
    )
    middle_grad, gain_two, shift_two = norm_backward(
        act_two_grad * swish_slope(pre_two), normed_two, inverse_two, norm_gains[1], members
    )
    grad_one = middle_grad.astype(jnp.bfloat16).reshape(grid_shape)
    act_one_grad, weight_one_grad, bias_one_grad = conv_backward(
        grad_one, row_mask, conv_weights[0], taps_one
    )
    input_back, gain_one, shift_one = norm_backward(
        act_one_grad * swish_slope(pre_one), normed_one, inverse_one, norm_gains[0], members
    )
    input_grad = residual_grad + input_back
    conv_grad = jnp.stack([weight_one_grad, weight_two_grad])
    conv_part = lax.psum_scatter(conv_grad, "height", scatter_dimension=4, tiled=True)
    conv_part = lax.psum_scatter(
        conv_part.astype(jnp.bfloat16), "canvas", scatter_dimension=3, tiled=True
    ).astype(jnp.float32)
    summed = lax.psum(
        (
            jnp.stack([gain_one, gain_two, gain_three]),
            jnp.stack([shift_one, shift_two, shift_three]),
            jnp.stack([bias_one_grad, bias_two_grad]),
            qkv_grad,
            qv_grad,
            proj_grad,
            proj_bias_grad,
        ),
        ("canvas", "height"),
    )
    return (
        output.astype(jnp.bfloat16).reshape((1,) + grid_shape),
        input_grad.astype(jnp.bfloat16).reshape((1,) + grid_shape),
        summed[0],
        summed[1],
        conv_part,
        summed[2],
        summed[3],
        summed[4],
        summed[5],
        summed[6],
    )


def fold(block):
    rows, width = block.shape
    return jnp.sum(block.reshape(rows // 8, 8, width), axis=0)


def group_lanes(block, group):
    lane = lax.broadcasted_iota(jnp.int32, block.shape, 1)
    width = block.shape[1]
    step = 1
    while step < group:
        above = pltpu.roll(block, step, 1)
        below = pltpu.roll(block, width - step, 1)
        block = block + jnp.where((lane & step) != 0, above, below)
        step *= 2
    return block


def group_mean(partial, members):
    spread = group_lanes(partial, partial.shape[1] // GROUPS)
    return jnp.sum(spread, axis=0, keepdims=True) * (1.0 / members)


def widen(block, width):
    return jnp.concatenate([block] * (width // block.shape[1]), axis=1)


def each_block(pixels, block, body, carry=0):
    def step(index, carry):
        return body(pl.ds(pl.multiple_of(index * block, block), block), carry)

    return lax.fori_loop(0, pixels // block, step, carry)


def each_chunk(pixels, body, carry):
    return each_block(pixels, CHUNK, body, carry)


def aligned(start, step):
    return start if isinstance(start, int) else pl.multiple_of(start, step)


class RunningStats:
    def __init__(self, channels):
        self.width = channels // GROUPS
        self.reference = None
        self.sums = self.squares = jnp.zeros((8, channels), jnp.float32)

    def add(self, block):
        if self.reference is None:
            self.reference = group_mean(block[0:8], 8.0 * self.width)
        offset = block - self.reference
        self.sums = self.sums + fold(offset)
        self.squares = self.squares + fold(offset * offset)

    def finish(self, pixels):
        both = group_lanes(jnp.concatenate([self.sums, self.squares], axis=0), self.width)
        share = 1.0 / (pixels * self.width)
        offset = column_total(both[0:8]) * share
        variance = column_total(both[8:16]) * share - offset * offset
        return self.reference + offset, lax.rsqrt(jnp.maximum(variance, 0.0) + epsilon)


def put_taps(taps_ref, block, rows, cols):
    count, channels = block.shape
    place = lax.broadcasted_iota(jnp.int32, block.shape, 0) & (cols - 1)
    left = jnp.where(place == 0, 0.0, pltpu.roll(block, 1, 0))
    right = jnp.where(place == cols - 1, 0.0, pltpu.roll(block, count - 1, 0))
    inner = pl.ds(aligned(rows.start + cols, cols), count)
    taps_ref[inner, 0:channels] = left.astype(jnp.bfloat16)
    taps_ref[inner, channels : 2 * channels] = block.astype(jnp.bfloat16)
    taps_ref[inner, 2 * channels :] = right.astype(jnp.bfloat16)


def clear_edges(taps_ref, cols):
    edge = jnp.zeros((cols, taps_ref.shape[1]), taps_ref.dtype)
    taps_ref[0:cols, :] = edge
    taps_ref[taps_ref.shape[0] - cols :, :] = edge


def begin_conv(taps_ref, product, total_ref, fill, first, cols):
    for start in range(0, total_ref.shape[0], FILL_ROWS):
        for inner in range(start, start + FILL_ROWS, CHUNK):
            fill(pl.ds(inner, CHUNK))
        rows = pl.ds(start, FILL_ROWS)
        total_ref[rows, :] = first(rows, product(taps_ref, pl.ds(start + cols, FILL_ROWS), 1))


def add_rows(taps_ref, product, mask_ref, total_ref, row_tap, last, cols, old_ref=None):
    pixels, channels = total_ref.shape
    old_ref = total_ref if old_ref is None else old_ref
    for start in range(0, pixels, FILL_ROWS):
        rows = slice(start, start + FILL_ROWS)
        part = product(taps_ref, pl.ds(start + row_tap * cols, FILL_ROWS), row_tap)
        mask = widen(mask_ref[row_tap // 2, rows, :], channels)
        total_ref[rows, :] = last(rows, old_ref[rows, :] + mask * part)


def run_conv(taps_ref, product, mask_ref, total_ref, fill, first, last, cols):
    begin_conv(taps_ref, product, total_ref, fill, first, cols)
    add_rows(taps_ref, product, mask_ref, total_ref, 0, lambda rows, value: value, cols)
    add_rows(taps_ref, product, mask_ref, total_ref, 2, last, cols)


def product_forward(weight_ref):
    channels = weight_ref.shape[-1]

    def product(taps_ref, shifted, row_tap):
        return jnp.dot(
            taps_ref[shifted, :],
            weight_ref[row_tap].reshape(3 * channels, channels),
            preferred_element_type=jnp.float32,
        )

    return product


def product_backward(weight_ref):
    def product(taps_ref, shifted, row_tap):
        return lax.dot_general(
            taps_ref[shifted, :],
            weight_ref[row_tap],
            (((1,), (1,)), ((), ())),
            preferred_element_type=jnp.float32,
        )

    return product


def activation(read, mean, inverse, gain, shift, act_ref, taps_ref, cols):
    scale, offset = 0.5 * inverse * gain, 0.5 * shift

    def fill(rows):
        half = (read(rows) - mean) * scale + offset
        act = half * (1.0 + jnp.tanh(half))
        act_ref[rows, :] = act.astype(jnp.bfloat16)
        put_taps(taps_ref, act, rows, cols)

    return fill


def back_means(sums, gain, pixels):
    channels = gain.shape[1]
    members = float(pixels * (channels // GROUPS))
    return group_mean(sums[0] * gain, members), group_mean(sums[1] * gain, members)


def column_total(partial):
    return jnp.sum(partial, axis=0, keepdims=True)


def weight_part(act_ref, grad_ref, lanes_ref, flip_ref, columns_ref, part_ref, cols):
    pixels, channels = act_ref.shape
    height = lax.axis_index("height")
    share = NARROW // 2
    block = pl.ds(pl.multiple_of((height // 2) * NARROW, NARROW), NARROW)
    flip_ref[...] = grad_ref[:, block].T
    own = pl.ds(pl.multiple_of((height % 2) * share, share), share)
    grad = flip_ref[own, :].astype(jnp.float32)
    column = lax.broadcasted_iota(jnp.int32, grad.shape, 1) & (cols - 1)
    for col_tap in range(3):
        shifted = grad
        if col_tap == 0:
            shifted = jnp.where(column == cols - 1, 0.0, pltpu.roll(grad, pixels - 1, 1))
        elif col_tap == 2:
            shifted = jnp.where(column == 0, 0.0, pltpu.roll(grad, 1, 1))
        for row_tap in range(3):
            tap = 3 * row_tap + col_tap
            place = slice(tap * share, (tap + 1) * share)
            if row_tap == 1:
                columns_ref[place, :] = shifted.astype(jnp.bfloat16)
                continue
            side, turn = (0, pixels - cols) if row_tap == 0 else (1, cols)
            masked = (shifted * lanes_ref[side : side + 1, :]).astype(jnp.bfloat16)
            columns_ref[place, :] = pltpu.roll(masked, turn, 1)
    part_ref[...] = jnp.dot(
        columns_ref[...], act_ref[...], preferred_element_type=jnp.float32
    ).astype(jnp.bfloat16)


def begin_back(grad_ref, weights_ref, mask_ref, taps_ref, total_ref, cols):
    clear_edges(taps_ref, cols)

    def fill(rows):
        put_taps(taps_ref, grad_ref[rows, :].astype(jnp.float32), rows, cols)

    product = product_backward(weights_ref)
    begin_conv(taps_ref, product, total_ref, fill, lambda rows, part: part, cols)
    add_rows(taps_ref, product, mask_ref, total_ref, 0, lambda rows, value: value, cols)


def finish_back(
    weights_ref, mask_ref, taps_ref, total_ref, read, table_ref, which, cols, old_ref=None
):
    mean, inverse, gain, shift = norm_rows(table_ref, which)
    scale, offset = 0.5 * inverse * gain, 0.5 * shift
    sums = []

    def slope(rows, value):
        centered = read(rows) - mean
        half = centered * scale + offset
        turn = jnp.tanh(half)
        double = value * ((1.0 + turn) * (1.0 + half * (1.0 - turn)))
        sums.append((fold(double), fold(double * centered)))
        return double

    add_rows(
        taps_ref, product_backward(weights_ref), mask_ref, total_ref, 2, slope, cols, old_ref
    )
    plain, cross = sum(pair[0] for pair in sums), sum(pair[1] for pair in sums)
    return 0.5 * plain, 0.5 * inverse * cross


def norm_back(total_ref, double, sums, read, table_ref, which, pixels):
    mean, inverse, gain, shift = norm_rows(table_ref, which)
    mean_grad, mean_cross = back_means(sums, gain, pixels)
    slope = inverse * gain * (0.5 if double else 1.0)
    level, tilt = inverse * mean_grad, inverse * inverse * mean_cross

    def back(rows, inner):
        return total_ref[inner, :] * slope - level - (read(rows) - mean) * tilt

    return back


def turn_kernel(
    grad_ref, mask_ref, weights_ref, middle_ref, table_ref, total_ref, sums_ref, taps_ref, *, cols
):
    begin_back(grad_ref, weights_ref.at[1], mask_ref, taps_ref, total_ref, cols)
    sums_ref[0:8, :], sums_ref[8:16, :] = finish_back(
        weights_ref.at[1],
        mask_ref,
        taps_ref,
        total_ref,
        lambda rows: middle_ref[rows, :],
        table_ref,
        1,
        cols,
    )


def norm_rows(table_ref, which):
    picks = (2 * which, 2 * which + 1, 6 + which, 9 + which)
    return tuple(table_ref[pick : pick + 1, :] for pick in picks)


def build_masks(ids_ref, mask_ref, lanes_ref, id_rows_ref, id_cols_ref, cols):
    rows = ids_ref.shape[1]
    for row in range(rows):
        here = ids_ref[0, row]
        place = slice(row * cols, (row + 1) * cols)
        id_rows_ref[place, :] = jnp.full((cols, LANES), here, jnp.int32)
        for side, other in ((0, row - 1), (1, row + 1)):
            same = jnp.float32(0.0)
            if 0 <= other < rows:
                same = jnp.where(ids_ref[0, other] == here, 1.0, 0.0).astype(jnp.float32)
            mask_ref[side, place, :] = jnp.full((cols, LANES), same, jnp.float32)
    lane = lax.broadcasted_iota(jnp.int32, (8, LANES), 1)
    each = LANES // cols
    for block in range(rows // each):
        ids = jnp.full((8, LANES), ids_ref[0, block * each], jnp.int32)
        for step in range(1, each):
            ids = jnp.where(lane >= step * cols, ids_ref[0, block * each + step], ids)
        id_cols_ref[:, block * LANES : (block + 1) * LANES] = ids
    ids = id_cols_ref[...].astype(jnp.float32)
    pixels = ids.shape[1]
    pixel = lax.broadcasted_iota(jnp.int32, ids.shape, 1)
    above = jnp.where(pixel < cols, -1.0, pltpu.roll(ids, cols, 1))
    below = jnp.where(pixel >= pixels - cols, -1.0, pltpu.roll(ids, pixels - cols, 1))
    lanes_ref[0:1, :] = jnp.where(above == ids, 1.0, 0.0)[0:1]
    lanes_ref[1:2, :] = jnp.where(below == ids, 1.0, 0.0)[0:1]


def place_pieces(pieces, whole_ref, sems):
    own_pixels = whole_ref.shape[0] // len(pieces)
    height = lax.axis_index("height")
    copies = []
    for place, piece in enumerate(pieces):
        start = pl.multiple_of((height ^ place) * own_pixels, own_pixels)
        rows = pl.ds(start, own_pixels)
        copies.append(pltpu.make_async_copy(piece, whole_ref.at[rows, :], sems.at[place]))
    return copies


def hold_kernel(
    ids_hbm,
    gains_hbm,
    shifts_hbm,
    biases_hbm,
    weights_hbm,
    qkv_hbm,
    proj_hbm,
    qv_bias_hbm,
    proj_bias_hbm,
    weights_ref,
    turned_ref,
    qkv_ref,
    proj_ref,
    table_ref,
    mask_ref,
    lanes_ref,
    id_rows_ref,
    id_cols_ref,
    ids_ref,
    gains_ref,
    shifts_ref,
    biases_ref,
    qv_bias_ref,
    proj_bias_ref,
    sems,
    *,
    cols,
):
    channels = weights_ref.shape[-1]
    small = [
        (ids_hbm, ids_ref),
        (gains_hbm, gains_ref),
        (shifts_hbm, shifts_ref),
        (biases_hbm, biases_ref),
        (qv_bias_hbm, qv_bias_ref),
        (proj_bias_hbm, proj_bias_ref),
    ]
    large = [(weights_hbm, weights_ref), (qkv_hbm, qkv_ref), (proj_hbm, proj_ref)]
    for which in range(2):
        for row_tap in range(3):
            for col_tap in range(3):
                place = slice(col_tap * channels, (col_tap + 1) * channels)
                large.append(
                    (
                        weights_hbm.at[which, 2 - row_tap, 2 - col_tap],
                        turned_ref.at[which, row_tap, :, place],
                    )
                )
    copies = [
        pltpu.make_async_copy(source, target, sems.at[index])
        for index, (source, target) in enumerate(small + large)
    ]
    for copy in copies:
        copy.start()
    for copy in copies[: len(small)]:
        copy.wait()
    build_masks(ids_ref, mask_ref, lanes_ref, id_rows_ref, id_cols_ref, cols)
    table_ref[6:9, :] = gains_ref[...]
    table_ref[9:12, :] = shifts_ref[...]
    table_ref[12:14, :] = biases_ref[...]
    table_ref[14:16, :] = qv_bias_ref[...]
    table_ref[16:17, :] = proj_bias_ref[...]
    for copy in copies[len(small) :]:
        copy.wait()


def conv_kernel(*refs, cols, count):
    pieces, refs = refs[:count], refs[count:]
    (
        weights_ref,
        params_ref,
        mask_ref,
        features_ref,
        act_one_ref,
        middle_ref,
        act_two_ref,
        residual_ref,
        table_ref,
        own_ref,
        taps_ref,
        sem,
    ) = refs
    pixels, channels = features_ref.shape
    wide = jnp.float32
    own_copy = pltpu.make_async_copy(pieces[0], own_ref, sem)
    own_copy.start()
    table_ref[...] = params_ref[...]
    clear_edges(taps_ref, cols)

    def read_input(rows):
        return features_ref[rows, :].astype(wide)

    def read_middle(rows):
        return middle_ref[rows, :]

    height = lax.axis_index("height")
    own_pixels = pixels // count
    seen = RunningStats(channels)
    for place in list(range(1, count)) + [0]:
        if place == 0:
            own_copy.wait()
        piece = (pieces[place] if place else own_ref)[...]
        start = pl.multiple_of((height ^ place) * own_pixels, own_pixels)
        features_ref[pl.ds(start, own_pixels), :] = piece
        seen.add(piece.astype(wide))
    table_ref[0:1, :], table_ref[1:2, :] = seen.finish(pixels)
    seen = RunningStats(channels)

    def keep(rows, value):
        seen.add(value)
        return value

    run_conv(
        taps_ref,
        product_forward(weights_ref.at[0]),
        mask_ref,
        middle_ref,
        activation(read_input, *norm_rows(table_ref, 0), act_one_ref, taps_ref, cols),
        lambda rows, part: part + table_ref[12:13, :],
        keep,
        cols,
    )
    table_ref[2:3, :], table_ref[3:4, :] = seen.finish(pixels)
    seen = RunningStats(channels)
    run_conv(
        taps_ref,
        product_forward(weights_ref.at[1]),
        mask_ref,
        residual_ref,
        activation(read_middle, *norm_rows(table_ref, 1), act_two_ref, taps_ref, cols),
        lambda rows, part: part + (read_input(rows) + table_ref[13:14, :]),
        keep,
        cols,
    )
    table_ref[4:5, :], table_ref[5:6, :] = seen.finish(pixels)


def score_kernel(
    qkv_ref,
    proj_ref,
    residual_ref,
    table_ref,
    id_rows_ref,
    id_cols_ref,
    normed_ref,
    query_ref,
    key_ref,
    value_ref,
    soft_ref,
    out_flip_ref,
    output_ref,
    value_flip_ref,
    *scores_refs,
    score_scale,
):
    pixels, channels = residual_ref.shape
    own_pixels = output_ref.shape[0]
    wide = jnp.float32
    exponent = score_scale * 1.4426950408889634
    mean, inverse, gain, shift = norm_rows(table_ref, 2)
    scale = inverse * gain

    def project(rows, carry):
        normed = ((residual_ref[rows, :] - mean) * scale + shift).astype(jnp.bfloat16)
        normed_ref[rows, :] = normed
        query_ref[rows, :] = (
            jnp.dot(normed, qkv_ref[:, 0:channels], preferred_element_type=wide)
            + table_ref[14:15, :]
        ).astype(jnp.bfloat16)
        key_ref[rows, :] = jnp.dot(
            normed, qkv_ref[:, channels : 2 * channels], preferred_element_type=wide
        ).astype(jnp.bfloat16)
        values = (
            jnp.dot(normed, qkv_ref[:, 2 * channels :], preferred_element_type=wide)
            + table_ref[15:16, :]
        ).astype(jnp.bfloat16)
        value_ref[rows, :] = values
        value_flip_ref[:, rows] = values.T
        return carry

    each_block(pixels, min(QUERY_ROWS, pixels), project)
    block = scores_refs[0].shape[1]
    steps = range(0, pixels, KEY_ROWS)

    def score(index):
        rows = slice(index * block, (index + 1) * block)
        for start in steps:
            keys = slice(start, start + KEY_ROWS)
            scores = lax.dot_general(
                key_ref[keys, :],
                query_ref[rows, :],
                (((1,), (1,)), ((), ())),
                preferred_element_type=wide,
            )
            same = widen(id_rows_ref[keys, :], block) == id_cols_ref[0:1, rows]
            scores_refs[index][keys, :] = jnp.where(same, scores, masked_score)

    def soften(index):
        rows = slice(index * block, (index + 1) * block)
        scores_ref = scores_refs[index]
        peak = jnp.full((8, block), masked_score, wide)
        for start in steps:
            scores = scores_ref[start : start + KEY_ROWS, :]
            peak = jnp.maximum(peak, jnp.max(scores.reshape(-1, 8, block), axis=0))
        peak = jnp.max(peak, axis=0, keepdims=True)
        total = jnp.zeros((8, block), wide)
        for start in steps:
            keys = slice(start, start + KEY_ROWS)
            powers = jnp.exp2((scores_ref[keys, :] - peak) * exponent)
            scores_ref[keys, :] = powers
            total = total + fold(powers)
        share = 1.0 / column_total(total)
        for start in steps:
            keys = slice(start, start + KEY_ROWS)
            soft_ref[keys, rows] = (scores_ref[keys, :] * share).astype(jnp.bfloat16)

    score(0)
    for index in range(len(scores_refs)):
        if index + 1 < len(scores_refs):
            score(index + 1)
        soften(index)

    def collect(rows, carry):
        out_flip_ref[rows, :] = jnp.dot(
            value_flip_ref[rows, :], soft_ref[...], preferred_element_type=wide
        ).astype(jnp.bfloat16)
        return carry

    each_block(channels, channels // 2, collect)
    height = lax.axis_index("height")
    own = pl.ds(pl.multiple_of(height * own_pixels, own_pixels), own_pixels)
    output_ref[...] = (
        residual_ref[own, :]
        + lax.dot_general(
            out_flip_ref[:, own],
            proj_ref[...],
            (((0,), (0,)), ((), ())),
            preferred_element_type=wide,
        )
        + table_ref[16:17, :]
    ).astype(jnp.bfloat16)


def own_quarter():
    height = lax.axis_index("height")
    return (height & 1) * 2 + ((height >> 1) & 1)


def send_order(source_ref, targets, axis, share):
    me = lax.axis_index("canvas")
    for step, target in enumerate(targets):
        place = pl.ds(pl.multiple_of((me ^ step) * share, share), share)
        target[...] = source_ref[place, :] if axis == 0 else source_ref[:, place]


def attention_kernel(
    proj_ref,
    normed_ref,
    query_ref,
    key_ref,
    value_ref,
    soft_ref,
    out_flip_ref,
    *refs,
    score_scale,
    count,
):
    pieces, (grad_ref, packed_ref, sums_ref), refs = (
        refs[:count],
        refs[count : count + 3],
        refs[count + 3 :],
    )
    pixels, channels = normed_ref.shape
    blocks = pixels // SCORE_ROWS
    grads_refs, refs = refs[-blocks:], refs[:-blocks]
    *mixed_refs, mixed_ref, key_flip_ref, back_ref, score_grad_ref, flip_ref, sems = refs
    wide = jnp.float32
    copies = place_pieces(pieces, grad_ref, sems)
    for copy in copies:
        copy.start()
    quarter = channels // 4
    own = pl.ds(pl.multiple_of(own_quarter() * quarter, quarter), quarter)
    flip_ref[...] = normed_ref[:, own].T
    key_flip_ref[...] = key_ref[...].T
    for copy in copies:
        copy.wait()
    block, count = SCORE_ROWS, blocks
    steps = range(0, pixels, KEY_ROWS)

    def block_rows(index):
        return slice(index * block, (index + 1) * block)

    for index in range(count):
        back_ref[block_rows(index), :] = lax.dot_general(
            grad_ref[block_rows(index), :],
            proj_ref[...],
            (((1,), (1,)), ((), ())),
            preferred_element_type=wide,
        ).astype(jnp.bfloat16)

    def weigh(index):
        total = jnp.zeros((8, block), wide)
        for start in steps:
            keys = slice(start, start + KEY_ROWS)
            weight_grad = lax.dot_general(
                value_ref[keys, :],
                back_ref[block_rows(index), :],
                (((1,), (1,)), ((), ())),
                preferred_element_type=wide,
            )
            grads_refs[index][keys, :] = weight_grad
            total = total + fold(soft_ref[keys, block_rows(index)].astype(wide) * weight_grad)
        return column_total(total)

    def slope(index, dots):
        for start in steps:
            keys = slice(start, start + KEY_ROWS)
            weights = soft_ref[keys, block_rows(index)].astype(wide)
            score_grad_ref[keys, block_rows(index)] = (
                weights * (grads_refs[index][keys, :] - dots)
            ).astype(jnp.bfloat16)

    dots = weigh(0)
    for index in range(count):
        now, rows = dots, block_rows(index)
        if index + 1 < count:
            dots = weigh(index + 1)
        slope(index, now)
        packed_ref[rows, 2 * channels :] = jnp.dot(
            soft_ref[rows, :], back_ref[...], preferred_element_type=wide
        ).astype(jnp.bfloat16)
        query_grad = jnp.dot(
            key_flip_ref[...], score_grad_ref[:, rows], preferred_element_type=wide
        )
        packed_ref[rows, 0:channels] = (query_grad * score_scale).astype(jnp.bfloat16).T
    for index in range(count):
        rows = block_rows(index)
        packed_ref[rows, channels : 2 * channels] = (
            jnp.dot(score_grad_ref[rows, :], query_ref[...], preferred_element_type=wide)
            * score_scale
        ).astype(jnp.bfloat16)

    def pack(rows, carry):
        return (
            carry[0] + fold(packed_ref[rows, 0:channels].astype(wide)),
            carry[1] + fold(packed_ref[rows, 2 * channels :].astype(wide)),
            carry[2] + fold(grad_ref[rows, :].astype(wide)),
        )

    zeros = jnp.zeros((8, channels), wide)
    totals = zeros, zeros, zeros
    for start in range(0, pixels, CHUNK):
        totals = pack(pl.ds(start, CHUNK), totals)
    sums_ref[...] = jnp.zeros(sums_ref.shape, wide)
    for row, total in enumerate(totals):
        sums_ref[8 + row : 9 + row, :] = column_total(total)
    mixed_ref[:, 0 : 3 * channels] = jnp.dot(
        flip_ref[...], packed_ref[...], preferred_element_type=wide
    ).astype(jnp.bfloat16)
    mixed_ref[:, 3 * channels :] = jnp.dot(
        out_flip_ref[own, :], grad_ref[...], preferred_element_type=wide
    ).astype(jnp.bfloat16)
    send_order(mixed_ref, mixed_refs, 0, quarter // len(mixed_refs))


def third_kernel(
    qkv_ref,
    grad_ref,
    packed_ref,
    residual_ref,
    table_ref,
    act_two_ref,
    lanes_ref,
    old_sums_ref,
    residual_grad_ref,
    grad_two_ref,
    sums_ref,
    keep_ref,
    send_ref,
    total_ref,
    flip_ref,
    columns_ref,
    part_ref,
    *,
    cols,
):
    pixels, channels = residual_ref.shape
    block = FILL_ROWS
    wide = jnp.float32
    mean, inverse, gain, shift = norm_rows(table_ref, 2)
    zeros = jnp.zeros((8, channels), wide)

    sums = (zeros, zeros)
    for start in range(0, pixels, block):
        rows = pl.ds(start, block)
        normed_grad = lax.dot_general(
            packed_ref[rows, :], qkv_ref[...], (((1,), (1,)), ((), ())), preferred_element_type=wide
        )
        total_ref[rows, :] = normed_grad
        centered = residual_ref[rows, :] - mean
        sums = sums[0] + fold(normed_grad), sums[1] + fold(normed_grad * centered)
    sums = sums[0], sums[1] * inverse
    sums_ref[...] = old_sums_ref[...]
    sums_ref[5:6, :] = column_total(sums[1])
    sums_ref[6:7, :] = column_total(sums[0])
    back = norm_back(
        total_ref, False, sums, lambda rows: residual_ref[rows, :], table_ref, 2, pixels
    )

    def finish(rows, carry):
        total = grad_ref[rows, :].astype(wide) + back(rows, rows)
        residual_grad_ref[rows, :] = total
        low = total.astype(jnp.bfloat16)
        grad_two_ref[rows, :] = low
        return carry + fold(low.astype(wide))

    sums_ref[7:8, :] = column_total(each_chunk(pixels, finish, zeros))
    weight_part(act_two_ref, grad_two_ref, lanes_ref, flip_ref, columns_ref, part_ref, cols)
    keep_half(part_ref, 2, 1, keep_ref, send_ref)


def second_kernel(
    total_ref,
    partial_ref,
    middle_ref,
    table_ref,
    act_one_ref,
    lanes_ref,
    old_sums_ref,
    grad_one_ref,
    sums_ref,
    keep_ref,
    send_ref,
    flip_ref,
    columns_ref,
    part_ref,
    *,
    cols,
):
    pixels, channels = middle_ref.shape
    sums = partial_ref[0:8, :], partial_ref[8:16, :]
    back = norm_back(
        total_ref, True, sums, lambda rows: middle_ref[rows, :], table_ref, 1, pixels
    )
    sums_ref[...] = old_sums_ref[...]
    sums_ref[2:3, :] = column_total(sums[1])
    sums_ref[3:4, :] = column_total(sums[0])

    def finish(rows, carry):
        low = back(rows, rows).astype(jnp.bfloat16)
        grad_one_ref[rows, :] = low
        return carry + fold(low.astype(jnp.float32))

    zeros = jnp.zeros((8, channels), jnp.float32)
    sums_ref[4:5, :] = column_total(each_chunk(pixels, finish, zeros))
    weight_part(act_one_ref, grad_one_ref, lanes_ref, flip_ref, columns_ref, part_ref, cols)
    keep_half(part_ref, 1, 2, keep_ref, send_ref)


def keep_half(part_ref, near, far, keep_ref, send_ref):
    me = lax.axis_index("canvas")
    rows, width = part_ref.shape[0], keep_ref.shape[1]
    for target_ref, flip in ((keep_ref, 0), (send_ref, near)):
        for slot in range(2):
            owner = me ^ flip ^ (slot * far)
            place = pl.ds(pl.multiple_of(owner * width, width), width)
            target_ref[slot * rows : (slot + 1) * rows, :] = part_ref[:, place]


def first_kernel(
    grad_one_ref,
    features_ref,
    table_ref,
    mask_ref,
    old_sums_ref,
    weights_ref,
    own_ref,
    sums_ref,
    partial_ref,
    total_ref,
    taps_ref,
    *,
    cols,
):
    def read(rows):
        return features_ref[rows, :].astype(jnp.float32)

    weights = weights_ref.at[0]
    begin_back(grad_one_ref, weights, mask_ref, taps_ref, total_ref, cols)
    sums = finish_back(weights, mask_ref, taps_ref, total_ref, read, table_ref, 0, cols)
    partial_ref[0:8, :], partial_ref[8:16, :] = sums
    sums_ref[...] = old_sums_ref[...]
    sums_ref[0:1, :] = column_total(sums[1])
    sums_ref[1:2, :] = column_total(sums[0])
    count = own_ref.shape[0]
    own = pl.ds(pl.multiple_of(lax.axis_index("height") * count, count), count)
    own_ref[...] = total_ref[own, :]


def own_kernel(
    own_ref, partial_ref, features_ref, residual_grad_ref, table_ref, input_grad_ref
):
    def read(rows):
        return features_ref[rows, :].astype(jnp.float32)

    sums = partial_ref[0:8, :], partial_ref[8:16, :]
    pixels = features_ref.shape[0]
    back = norm_back(own_ref, True, sums, read, table_ref, 0, pixels)
    count = own_ref.shape[0]
    own = pl.ds(pl.multiple_of(lax.axis_index("height") * count, count), count)
    total = residual_grad_ref[own, :] + back(own, slice(0, count))
    input_grad_ref[...] = total.astype(jnp.bfloat16)


def place_kernel(*refs):
    joints, packed_ref = refs[:-1], refs[-1]
    share = packed_ref.shape[0] // len(joints)
    me = lax.axis_index("canvas")
    for step, joint in enumerate(joints):
        place = pl.ds(pl.multiple_of((me ^ step) * share, share), share)
        packed_ref[place, :] = joint[...]


def spread_quarters(packed, flips, qkv_ref, proj_ref, qkv_hbm, proj_hbm, sems):
    quarter = packed[0].shape[0]
    inner = qkv_ref.shape[2]
    copies = []
    for index, packed_ref in enumerate(packed):
        owner = own_quarter() ^ flips[index]
        rows = pl.ds(pl.multiple_of(owner * quarter, quarter), quarter)
        qkv_ref[index] = packed_ref[:, 0:inner].astype(jnp.float32)
        proj_ref[index] = packed_ref[:, inner:].astype(jnp.float32)
        for which, (held, target) in enumerate(((qkv_ref, qkv_hbm), (proj_ref, proj_hbm))):
            copy = pltpu.make_async_copy(held.at[index], target.at[rows, :], sems.at[index, which])
            copy.start()
            copies.append(copy)
    return copies


def join_kernel(*refs):
    packed, (qkv_hbm, proj_hbm, qkv_ref, proj_ref, sems) = refs[:-5], refs[-5:]
    copies = spread_quarters(
        packed, range(len(packed)), qkv_ref, proj_ref, qkv_hbm, proj_hbm, sems
    )
    for copy in copies:
        copy.wait()


def halve_kernel(keep_ref, got_ref, hold_ref, send_ref):
    total = keep_ref[...].astype(jnp.float32) + got_ref[...].astype(jnp.float32)
    rows = hold_ref.shape[0]
    hold_ref[...] = total[0:rows]
    send_ref[0:rows, :] = total[rows:].astype(jnp.bfloat16)


def halve_sums_kernel(
    keep_one_ref,
    got_one_ref,
    keep_two_ref,
    got_two_ref,
    sums_ref,
    hold_ref,
    send_ref,
    hold_two_ref,
    send_two_ref,
):
    halve_kernel(keep_one_ref, got_one_ref, hold_ref, send_ref)
    halve_kernel(keep_two_ref, got_two_ref, hold_two_ref, send_two_ref)
    rows = hold_ref.shape[0]
    left = sums_ref[...]
    count, width = left.shape
    for part in range(2):
        low = left.astype(jnp.bfloat16)
        left = left - low.astype(jnp.float32)
        for block in range(width // LANES):
            send_ref[rows : rows + count, :] = low[:, block * LANES : (block + 1) * LANES]
            rows += count


def unpack_sums(got_ref, rows, count, width):
    total = jnp.zeros((count, width), jnp.float32)
    for part in range(2):
        blocks = []
        for block in range(width // LANES):
            blocks.append(got_ref[rows : rows + count, :].astype(jnp.float32))
            rows += count
        total = total + jnp.concatenate(blocks, axis=1)
    return total


def sums_kernel(
    sums_ref,
    near_ref,
    far_ref,
    hold_one_ref,
    got_one_ref,
    hold_two_ref,
    got_two_ref,
    share_ref,
    gains_ref,
    shifts_ref,
    conv_ref,
    qv_ref,
    bias_ref,
):
    rows = hold_one_ref.shape[0]
    for which, (hold_ref, got_ref) in enumerate(
        ((hold_one_ref, got_one_ref), (hold_two_ref, got_two_ref))
    ):
        total = hold_ref[...] + got_ref[0:rows, :].astype(jnp.float32)
        share_ref[which] = total.reshape(share_ref.shape[1:])
    total = sums_ref[...] + near_ref[...] + far_ref[...]
    total = total + unpack_sums(got_one_ref, rows, *total.shape)
    for row, start in enumerate((0, 2, 5)):
        gains_ref[row : row + 1, :] = total[start : start + 1]
        shifts_ref[row : row + 1, :] = total[start + 1 : start + 2]
    conv_ref[0:1, :] = total[4:5]
    conv_ref[1:2, :] = total[7:8]
    qv_ref[...] = total[8:10]
    bias_ref[...] = total[10:11]


def call_kernel(kernel, outputs, scratch, operands, places, flops, limit, out_places=None, aliases={}):
    out_places = out_places or "v" * len(outputs)
    spaces = {
        "v": pl.BlockSpec(memory_space=pltpu.VMEM),
        "s": pl.BlockSpec(memory_space=pltpu.SMEM),
        "h": pl.BlockSpec(memory_space=pl.ANY),
        "o": pl.BlockSpec(memory_space=pltpu.VMEM),
        "a": pl.BlockSpec(memory_space=pl.ANY),
    }
    moved = 8 * flops // LANES
    held = {"v": pltpu.VMEM, "h": pltpu.HBM, "o": jax.ShapeDtypeStruct}
    operands = [
        pltpu.with_memory_space_constraint(array, pltpu.HBM) if place == "h" else array
        for array, place in zip(operands, places)
    ]
    return pl.pallas_call(
        kernel,
        out_shape=[held[place](*output) for output, place in zip(outputs, out_places)],
        in_specs=[spaces[place] for place in places],
        out_specs=[spaces[place] for place in out_places],
        scratch_shapes=scratch,
        input_output_aliases=aliases,
        compiler_params=pltpu.CompilerParams(vmem_limit_bytes=limit * 2**20),
        cost_estimate=pl.CostEstimate(flops=flops, bytes_accessed=moved, transcendentals=0),
    )(*operands)


def send_height(block, step):
    size = lax.axis_size("height")
    return lax.ppermute(block, "height", [(i, i ^ step) for i in range(size)])


def with_cores(blocks):
    return [piece for block in blocks for piece in (block, send_height(block, 1))]


def send_canvas(block, step):
    size = lax.axis_size("canvas")
    return lax.ppermute(block, "canvas", [(i, i ^ step) for i in range(size)])


def trade_canvas(pieces):
    return [pieces[0]] + [send_canvas(piece, step) for step, piece in enumerate(pieces) if step]


def whole_canvas(
    features,
    tile_ids,
    norm_gains,
    norm_shifts,
    conv_weights,
    conv_biases,
    qkv_weight,
    qv_bias,
    proj_weight,
    proj_bias,
    cotangent,
):
    height_size = lax.axis_size("height")
    canvas_size = lax.axis_size("canvas")
    local_rows, cols, channels = features.shape[1:]
    all_rows = tile_ids.shape[1]
    pixels = all_rows * cols
    own_pixels = local_rows * cols
    out_share = channels // height_size
    ci_share = channels // canvas_size
    quarter = channels // 4
    row_share = quarter // canvas_size
    low, wide = jnp.bfloat16, jnp.float32

    own_features = features.reshape(own_pixels, channels)
    own_grad = cotangent.reshape(own_pixels, channels)
    steps = range(2, height_size, 2)
    held_features = [own_features] + [send_height(own_features, step) for step in steps]
    plane = ((pixels, channels), low)
    plane_wide = ((pixels, channels), wide)
    sums_shape = ((16, channels), wide)
    mixed_shapes = [((row_share, 4 * channels), low)] * canvas_size
    taps = pltpu.VMEM((pixels + 2 * cols, 3 * channels), low)
    held_wide = pltpu.VMEM((pixels, channels), wide)
    flipped = pltpu.VMEM((channels, pixels), low)
    narrow = pltpu.VMEM((NARROW, pixels), low)
    columns = pltpu.VMEM((9 * out_share, pixels), low)
    part_held = pltpu.VMEM((9 * out_share, channels), low)
    sem = pltpu.SemaphoreType.DMA
    conv_flops = 2 * 9 * pixels * channels * channels
    dot_flops = 2 * pixels * channels * channels
    score_flops = 2 * pixels * pixels * channels
    scale = channels ** (-0.5)

    (
        held_conv,
        turned,
        held_qkv,
        held_proj,
        params,
        mask,
        lane_mask,
        id_rows,
        id_cols,
    ) = call_kernel(
        functools.partial(hold_kernel, cols=cols),
        [
            (conv_weights.shape, low),
            ((2, 3, channels, 3 * channels), low),
            (qkv_weight.shape, low),
            (proj_weight.shape, low),
            ((24, channels), wide),
            ((2, pixels, LANES), wide),
            ((8, pixels), wide),
            ((pixels, LANES), jnp.int32),
            ((8, pixels), jnp.int32),
        ],
        [
            pltpu.SMEM(tile_ids.shape, jnp.int32),
            pltpu.VMEM(norm_gains.shape, wide),
            pltpu.VMEM(norm_shifts.shape, wide),
            pltpu.VMEM(conv_biases.shape, wide),
            pltpu.VMEM(qv_bias.shape, wide),
            pltpu.VMEM((1, channels), wide),
            sem((27,)),
        ],
        [
            tile_ids,
            norm_gains,
            norm_shifts,
            conv_biases,
            conv_weights,
            qkv_weight,
            proj_weight,
            qv_bias,
            proj_bias.reshape(1, channels),
        ],
        "h" * 9,
        conv_flops,
        8,
    )
    held_features[1:] = [
        lax.optimization_barrier((params, block))[1] for block in held_features[1:]
    ]
    pieces = with_cores(held_features)
    far_grad, *pieces[4::2] = lax.optimization_barrier((own_grad, *held_features[2:]))
    held_grads = [own_grad, send_height(own_grad, 2)]
    held_grads[1], pieces[2] = lax.optimization_barrier((held_grads[1], held_features[1]))
    held_grads += [send_height(far_grad, step) for step in steps[1:]]

    all_features, act_one, middle, act_two, residual, table = call_kernel(
        functools.partial(conv_kernel, cols=cols, count=height_size),
        [plane, plane, plane_wide, plane, plane_wide, ((24, channels), wide)],
        [pltpu.VMEM((own_pixels, channels), low), taps, sem],
        [*pieces, held_conv, params, mask],
        "h" + "v" * (height_size + 2),
        2 * conv_flops,
        16,
    )
    residual, *held_grads = lax.optimization_barrier((residual, *held_grads))
    grad_pieces = with_cores(held_grads)
    normed, query, key, value, soft, out_flip, output = call_kernel(
        functools.partial(score_kernel, score_scale=scale),
        [
            plane,
            plane,
            plane,
            plane,
            ((pixels, pixels), low),
            ((channels, pixels), low),
            ((own_pixels, channels), low),
        ],
        [
            flipped,
            *[pltpu.VMEM((pixels, SCORE_ROWS), wide)] * (pixels // SCORE_ROWS),
        ],
        [
            held_qkv,
            held_proj,
            residual,
            table,
            id_rows,
            id_cols,
        ],
        "vvvvvv",
        3 * dot_flops + 2 * score_flops,
        20,
        "v" * 6 + "o",
    )
    normed, *grad_pieces = lax.optimization_barrier((normed, *grad_pieces))
    all_grad, packed, sums, *mixed = call_kernel(
        functools.partial(attention_kernel, score_scale=scale, count=height_size),
        [plane, ((pixels, 3 * channels), low), sums_shape, *mixed_shapes],
        [
            pltpu.VMEM((quarter, 4 * channels), low),
            flipped,
            pltpu.VMEM((pixels, channels), low),
            pltpu.VMEM((pixels, pixels), low),
            pltpu.VMEM((quarter, pixels), low),
            sem((height_size,)),
            *[pltpu.VMEM((pixels, SCORE_ROWS), wide)] * (pixels // SCORE_ROWS),
        ],
        [held_proj, normed, query, key, value, soft, out_flip, *grad_pieces],
        "vvvvvvvh" + "a" * (height_size - 1),
        3 * dot_flops + 4 * score_flops,
        20,
    )
    mixed = trade_canvas(mixed)
    halves = [((18 * out_share, ci_share), low)] * 2
    residual_grad, grad_two, sums, keep_two, send_two = call_kernel(
        functools.partial(third_kernel, cols=cols),
        [plane_wide, plane, sums_shape, *halves],
        [held_wide, narrow, columns, part_held],
        [held_qkv, all_grad, packed, residual, table, act_two, lane_mask, sums],
        "vvvvvvvv",
        3 * dot_flops + conv_flops // height_size,
        16,
    )
    grad_two, *mixed = lax.optimization_barrier((grad_two, *mixed))
    mixed_sum = mixed[0].astype(wide)
    for piece in mixed[1:]:
        mixed_sum = mixed_sum + piece.astype(wide)
    joints = trade_canvas([mixed_sum.astype(low)] * canvas_size)
    act_two_grad, partial_sums = call_kernel(
        functools.partial(turn_kernel, cols=cols),
        [plane_wide, sums_shape],
        [taps],
        [grad_two, mask, turned, middle, table],
        "vvvvv",
        conv_flops,
        16,
    )
    act_two_grad, *joints = lax.optimization_barrier((act_two_grad, *joints))
    (own_mixed,) = call_kernel(
        place_kernel,
        [((quarter, 4 * channels), low)],
        [],
        joints,
        "v" * canvas_size,
        1,
        12,
    )
    own_mixed, send_two = lax.optimization_barrier((own_mixed, send_two))
    got_two = send_canvas(send_two, 2)
    chip_mixed = send_height(own_mixed, 2)
    core_mixed = send_height(own_mixed, 1)
    grad_one, sums, keep_one, send_one = call_kernel(
        functools.partial(second_kernel, cols=cols),
        [plane, sums_shape, *halves],
        [narrow, columns, part_held],
        [act_two_grad, partial_sums, middle, table, act_one, lane_mask, sums],
        "vvvvvvv",
        1,
        16,
    )
    got_one = send_canvas(send_one, 1)

    own_total, sums, partial_sums = call_kernel(
        functools.partial(first_kernel, cols=cols),
        [((own_pixels, channels), wide), sums_shape, sums_shape],
        [held_wide, taps],
        [grad_one, all_features, table, mask, sums, turned],
        "vvvvvv",
        1,
        20,
    )
    share_rows = 9 * out_share
    send_rows = share_rows + 2 * sums_shape[0][0] * channels // LANES
    sums, core_mixed, got_one, got_two = lax.optimization_barrier(
        (sums, core_mixed, got_one, got_two)
    )
    hold_one, send_one, hold_two, send_two = call_kernel(
        halve_sums_kernel,
        [
            ((share_rows, ci_share), wide),
            ((send_rows, ci_share), low),
            ((share_rows, ci_share), wide),
            ((share_rows, ci_share), low),
        ],
        [],
        [keep_one, got_one, keep_two, got_two, sums],
        "vvvvv",
        1,
        12,
    )
    got_two = send_canvas(send_two, 1)
    got_one = send_canvas(send_one, 2)
    near_sums, far_sums = send_canvas(sums, 1), send_canvas(sums, 3)
    chip_mixed, hold_one = lax.optimization_barrier((chip_mixed, hold_one))
    both_mixed = send_height(chip_mixed, 1)
    own_total, hold_one = lax.optimization_barrier((own_total, hold_one))
    (input_grad,) = call_kernel(
        own_kernel,
        [((own_pixels, channels), low)],
        [],
        [own_total, partial_sums, all_features, residual_grad, table],
        "vvvvv",
        dot_flops // 4,
        12,
        "o",
    )
    input_grad, both_mixed = lax.optimization_barrier((input_grad, both_mixed))
    qkv_grad, proj_grad = call_kernel(
        join_kernel,
        [(qkv_weight.shape, wide), (proj_weight.shape, wide)],
        [
            pltpu.VMEM((4, quarter, 3 * channels), wide),
            pltpu.VMEM((4, quarter, channels), wide),
            sem((4, 2)),
        ],
        [own_mixed, chip_mixed, core_mixed, both_mixed],
        "vvvv",
        1,
        12,
        "hh",
    )
    qkv_grad, got_one, got_two, near_sums, far_sums = lax.optimization_barrier(
        (qkv_grad, got_one, got_two, near_sums, far_sums)
    )
    vector_shapes = [norm_gains.shape, norm_shifts.shape, conv_biases.shape, qv_bias.shape]
    conv_grad, gains_grad, shifts_grad, biases_grad, qv_grad, proj_bias_grad = call_kernel(
        sums_kernel,
        [((2, 3, 3, out_share, ci_share), wide)]
        + [(shape, wide) for shape in vector_shapes + [(1, channels)]],
        [],
        [sums, near_sums, far_sums, hold_one, got_one, hold_two, got_two],
        "vvvvvvv",
        1,
        12,
        "o" * 6,
    )
    own_shape = (1, local_rows, cols, channels)
    return (
        output.reshape(own_shape),
        input_grad.reshape(own_shape),
        gains_grad,
        shifts_grad,
        jnp.swapaxes(conv_grad, 3, 4),
        biases_grad,
        qkv_grad,
        qv_grad,
        proj_grad,
        proj_bias_grad.reshape(channels),
    )


def on_device(*arrays):
    features, tile_ids = arrays[0], arrays[1]
    local_rows, cols, channels = features.shape[1:]
    pixels = tile_ids.shape[1] * cols
    height_size, canvas_size = lax.axis_size("height"), lax.axis_size("canvas")
    powers = all(size & (size - 1) == 0 for size in (height_size, canvas_size, cols))
    fits = (
        powers
        and height_size > 2
        and canvas_size == 4
        and channels == LANES * canvas_size
        and pixels <= MOST_PIXELS
        and pixels % FILL_ROWS == 0
        and FILL_ROWS % CHUNK == 0
        and pixels % SCORE_ROWS == 0
        and pixels % KEY_ROWS == 0
        and (local_rows * cols) % LANES == 0
        and CHUNK % cols == 0
        and cols % 16 == 0
        and channels % (LANES * canvas_size) == 0
        and 2 * channels == NARROW * height_size
    )
    return whole_canvas(*arrays) if fits else split_canvas(*arrays)


def solution(mesh):
    in_specs = (
        P("canvas", "height", None, None),
        P("canvas", None),
        P(),
        P(),
        P(),
        P(),
        P(),
        P(),
        P(),
        P(),
        P("canvas", "height", None, None),
    )
    out_specs = (
        P("canvas", "height", None, None),
        P("canvas", "height", None, None),
        P(),
        P(),
        P(None, None, None, "canvas", "height"),
        P(),
        P(),
        P(),
        P(),
        P(),
    )
    return jax.shard_map(
        on_device, mesh=mesh, in_specs=in_specs, out_specs=out_specs, check_vma=False
    )
```

```python
import functools

import jax
import jax.numpy as jnp
from jax import lax
from jax.experimental import pallas as pl
from jax.experimental.pallas import tpu as pltpu
from jax.sharding import PartitionSpec as P

GROUPS = 32


epsilon = 1e-06
masked_score = -1e30
MOST_PIXELS = 1024
LANES = 128
NARROW = 128
CHUNK = 128
FILL_ROWS = 256
QUERY_ROWS = 512
SCORE_ROWS = 256
KEY_ROWS = 256


def extended(block, sides, width):
    for axis, dim in sides:
        count = lax.axis_size(axis)
        forward = [(i, i + 1) for i in range(count - 1)]
        backward = [(target, source) for source, target in forward]
        low = lax.ppermute(
            lax.slice_in_dim(block, block.shape[dim] - width, None, axis=dim), axis, forward
        )
        high = lax.ppermute(lax.slice_in_dim(block, 0, width, axis=dim), axis, backward)
        block = jnp.concatenate([low, block, high], axis=dim)
    return block


def group_total(vector):
    return vector.reshape(GROUPS, -1).sum(axis=1)


def spread_groups(vector, channels):
    return jnp.repeat(vector, channels // GROUPS)


def norm_forward(values, gain, shift, members):
    channels = values.shape[1]
    totals = lax.psum(group_total(jnp.sum(values, axis=0)), "height")
    centered = values - spread_groups(totals / members, channels)
    squares = lax.psum(group_total(jnp.sum(centered * centered, axis=0)), "height")
    inverse = spread_groups(lax.rsqrt(squares / members + epsilon), channels)
    normed = centered * inverse
    return (normed, inverse, normed * gain + shift)


def norm_backward(grad_in, normed, inverse, gain, members):
    channels = grad_in.shape[1]
    scaled = grad_in * gain
    both_sums = lax.psum(
        (group_total(jnp.sum(scaled, axis=0)), group_total(jnp.sum(scaled * normed, axis=0))),
        "height",
    )
    mean_grad = spread_groups(both_sums[0] / members, channels)
    mean_cross = spread_groups(both_sums[1] / members, channels)
    result = inverse * (scaled - mean_grad - normed * mean_cross)
    return (result, jnp.sum(grad_in * normed, axis=0), jnp.sum(grad_in, axis=0))


def swish(values):
    return values * jax.nn.sigmoid(values)


def swish_slope(values):
    sigmoid_part = jax.nn.sigmoid(values)
    return sigmoid_part * (1.0 + values * (1.0 - sigmoid_part))


def tap_columns(padded, row_mask, local_rows, canvas_cols):
    pieces = []
    for row_tap in range(3):
        rows_taken = padded[row_tap : row_tap + local_rows] * row_mask[:, row_tap, None, None]
        for col_tap in range(3):
            pieces.append(rows_taken[:, col_tap : col_tap + canvas_cols])
    stacked = jnp.concatenate(pieces, axis=2)
    return stacked.reshape(local_rows * canvas_cols, stacked.shape[2])


def conv_forward(acts, row_mask, weight, bias):
    local_rows, canvas_cols, channels = acts.shape
    rimmed = extended(acts, (("height", 0),), 1)
    padded = jnp.pad(rimmed, ((0, 0), (1, 1), (0, 0)))
    gathered = tap_columns(padded, row_mask, local_rows, canvas_cols)
    result = (
        jnp.dot(
            gathered, weight.reshape(9 * channels, channels), preferred_element_type=jnp.float32
        )
        + bias
    )
    return (result, gathered)


def conv_backward(grad_low, row_mask, weight, gathered):
    local_rows, canvas_cols, channels = grad_low.shape
    flat_grad = grad_low.reshape(local_rows * canvas_cols, channels)
    weight_grad = lax.dot_general(
        gathered, flat_grad, (((0,), (0,)), ((), ())), preferred_element_type=jnp.float32
    )
    rimmed = extended(grad_low, (("height", 0),), 1)
    padded = jnp.pad(rimmed, ((0, 0), (1, 1), (0, 0)))
    grad_taps = tap_columns(padded, row_mask, local_rows, canvas_cols)
    flipped = jnp.transpose(weight[::-1, ::-1], (0, 1, 3, 2)).reshape(9 * channels, channels)
    input_part = jnp.dot(grad_taps, flipped, preferred_element_type=jnp.float32)
    return (
        input_part,
        weight_grad.reshape(3, 3, channels, channels),
        jnp.sum(flat_grad.astype(jnp.float32), axis=0),
    )


def take_rows(array, offset, count):
    return lax.dynamic_slice_in_dim(array, offset, count)


def score_grads(
    queries, out_grad, log_total, row_dots, query_ids, key_rows, value_rows, key_ids, score_scale
):
    scores = (
        lax.dot_general(
            queries, key_rows, (((1,), (1,)), ((), ())), preferred_element_type=jnp.float32
        )
        * score_scale
    )
    same_tile = query_ids[:, None] == key_ids[None, :]
    softmax_block = jnp.exp(jnp.where(same_tile, scores - log_total[:, None], masked_score))
    weight_grad = lax.dot_general(
        out_grad, value_rows, (((1,), (1,)), ((), ())), preferred_element_type=jnp.float32
    )
    score_grad = (softmax_block * (weight_grad - row_dots[:, None])).astype(jnp.bfloat16)
    return (softmax_block.astype(jnp.bfloat16), score_grad)


def split_canvas(
    features,
    tile_ids,
    norm_gains,
    norm_shifts,
    conv_weights,
    conv_biases,
    qkv_weight,
    qv_bias,
    proj_weight,
    proj_bias,
    cotangent,
):
    height_size = lax.axis_size("height")
    local_rows = features.shape[1]
    canvas_cols = features.shape[2]
    channels = features.shape[3]
    pixels = local_rows * canvas_cols
    row_ids = tile_ids[0]
    all_rows = row_ids.shape[0]
    members = float(all_rows * canvas_cols * (channels // GROUPS))
    score_scale = channels ** (-0.5)
    first_row = lax.axis_index("height") * local_rows
    edge_ids = jnp.full((1,), -1, jnp.int32)
    padded_ids = jnp.concatenate([edge_ids, row_ids, edge_ids])
    near_ids = lax.dynamic_slice_in_dim(padded_ids, first_row, local_rows + 2)
    own_rows = near_ids[1 : local_rows + 1]
    row_mask = jnp.stack(
        [near_ids[row_tap : row_tap + local_rows] == own_rows for row_tap in range(3)], axis=1
    ).astype(jnp.bfloat16)
    key_ids = jnp.repeat(row_ids, canvas_cols)
    query_ids = jnp.repeat(own_rows, canvas_cols)
    grid_shape = (local_rows, canvas_cols, channels)
    inputs = features[0].reshape(pixels, channels).astype(jnp.float32)
    normed_one, inverse_one, pre_one = norm_forward(inputs, norm_gains[0], norm_shifts[0], members)
    act_one = swish(pre_one).astype(jnp.bfloat16).reshape(grid_shape)
    middle, taps_one = conv_forward(act_one, row_mask, conv_weights[0], conv_biases[0])
    normed_two, inverse_two, pre_two = norm_forward(middle, norm_gains[1], norm_shifts[1], members)
    act_two = swish(pre_two).astype(jnp.bfloat16).reshape(grid_shape)
    branch, taps_two = conv_forward(act_two, row_mask, conv_weights[1], conv_biases[1])
    residual = inputs + branch
    normed_three, inverse_three, pre_three = norm_forward(
        residual, norm_gains[2], norm_shifts[2], members
    )
    attn_input = pre_three.astype(jnp.bfloat16)
    mixed = jnp.dot(attn_input, qkv_weight, preferred_element_type=jnp.float32)
    queries = (mixed[:, :channels] + qv_bias[0]).astype(jnp.bfloat16)
    key_rows = mixed[:, channels : 2 * channels].astype(jnp.bfloat16)
    value_rows = (mixed[:, 2 * channels :] + qv_bias[1]).astype(jnp.bfloat16)
    running_max = jnp.full((pixels,), masked_score, jnp.float32)
    key_piece = lax.all_gather(key_rows, "height", axis=0, tiled=True)
    value_piece = lax.all_gather(value_rows, "height", axis=0, tiled=True)
    scores = (
        lax.dot_general(
            queries, key_piece, (((1,), (1,)), ((), ())), preferred_element_type=jnp.float32
        )
        * score_scale
    )
    same_tile = query_ids[:, None] == key_ids[None, :]
    scores = jnp.where(same_tile, scores, masked_score)
    new_max = jnp.maximum(running_max, jnp.max(scores, axis=1))
    weights = jnp.where(same_tile, jnp.exp(scores - new_max[:, None]), 0.0)
    summed_out = jnp.dot(
        weights.astype(jnp.bfloat16), value_piece, preferred_element_type=jnp.float32
    )
    total_weight = jnp.sum(weights, axis=1)
    log_total = new_max + jnp.log(total_weight)
    attended = summed_out / total_weight[:, None]
    attended_low = attended.astype(jnp.bfloat16)
    output = (
        residual
        + jnp.dot(attended_low, proj_weight, preferred_element_type=jnp.float32)
        + proj_bias
    )
    out_grad = cotangent[0].reshape(pixels, channels)
    out_grad_full = out_grad.astype(jnp.float32)
    proj_grad = lax.dot_general(
        attended_low, out_grad, (((0,), (0,)), ((), ())), preferred_element_type=jnp.float32
    )
    proj_bias_grad = jnp.sum(out_grad_full, axis=0)
    attended_grad = lax.dot_general(
        out_grad, proj_weight, (((1,), (1,)), ((), ())), preferred_element_type=jnp.float32
    ).astype(jnp.bfloat16)
    row_dots = jnp.sum(attended_grad.astype(jnp.float32) * attended, axis=1)
    block_rows = pixels * min(height_size, 8)
    zero_block = jnp.zeros((pixels, channels), jnp.float32)
    key_all, value_all = (
        lax.all_gather(key_rows, "height", axis=0, tiled=True),
        lax.all_gather(value_rows, "height", axis=0, tiled=True),
    )
    query_all, grad_all = (
        lax.all_gather(queries, "height", axis=0, tiled=True),
        lax.all_gather(attended_grad, "height", axis=0, tiled=True),
    )
    total_all, dots_all = (
        lax.all_gather(log_total, "height", axis=0, tiled=True),
        lax.all_gather(row_dots, "height", axis=0, tiled=True),
    )

    def own_query_step(running, block_index):
        offset = block_index * block_rows
        key_part = take_rows(key_all, offset, block_rows)
        rounded, score_grad = score_grads(
            queries,
            attended_grad,
            log_total,
            row_dots,
            query_ids,
            key_part,
            take_rows(value_all, offset, block_rows),
            take_rows(key_ids, offset, block_rows),
            score_scale,
        )
        return (
            running
            + jnp.dot(score_grad, key_part, preferred_element_type=jnp.float32) * score_scale,
            None,
        )

    def own_key_step(running, block_index):
        offset = block_index * block_rows
        query_part = take_rows(query_all, offset, block_rows)
        grad_part = take_rows(grad_all, offset, block_rows)
        rounded, score_grad = score_grads(
            query_part,
            grad_part,
            take_rows(total_all, offset, block_rows),
            take_rows(dots_all, offset, block_rows),
            take_rows(key_ids, offset, block_rows),
            key_rows,
            value_rows,
            query_ids,
            score_scale,
        )
        key_part = (
            lax.dot_general(
                score_grad, query_part, (((0,), (0,)), ((), ())), preferred_element_type=jnp.float32
            )
            * score_scale
        )
        value_part = lax.dot_general(
            rounded, grad_part, (((0,), (0,)), ((), ())), preferred_element_type=jnp.float32
        )
        return ((running[0] + key_part, running[1] + value_part), None)

    block_count = key_all.shape[0] // block_rows
    query_grad, unused_one = lax.scan(own_query_step, zero_block, jnp.arange(block_count))
    (key_grad, value_grad), unused_two = lax.scan(
        own_key_step, (zero_block, zero_block), jnp.arange(block_count)
    )
    query_low = query_grad.astype(jnp.bfloat16)
    key_low = key_grad.astype(jnp.bfloat16)
    value_low = value_grad.astype(jnp.bfloat16)
    stacked_grad = jnp.concatenate([query_low, key_low, value_low], axis=1)
    qkv_grad = lax.dot_general(
        attn_input, stacked_grad, (((0,), (0,)), ((), ())), preferred_element_type=jnp.float32
    )
    qv_grad = jnp.stack(
        [
            jnp.sum(query_low.astype(jnp.float32), axis=0),
            jnp.sum(value_low.astype(jnp.float32), axis=0),
        ]
    )
    normed_grad = lax.dot_general(
        stacked_grad, qkv_weight, (((1,), (1,)), ((), ())), preferred_element_type=jnp.float32
    )
    back_three, gain_three, shift_three = norm_backward(
        normed_grad, normed_three, inverse_three, norm_gains[2], members
    )
    residual_grad = out_grad_full + back_three
    grad_two = residual_grad.astype(jnp.bfloat16).reshape(grid_shape)
    act_two_grad, weight_two_grad, bias_two_grad = conv_backward(
        grad_two, row_mask, conv_weights[1], taps_two
    )
    middle_grad, gain_two, shift_two = norm_backward(
        act_two_grad * swish_slope(pre_two), normed_two, inverse_two, norm_gains[1], members
    )
    grad_one = middle_grad.astype(jnp.bfloat16).reshape(grid_shape)
    act_one_grad, weight_one_grad, bias_one_grad = conv_backward(
        grad_one, row_mask, conv_weights[0], taps_one
    )
    input_back, gain_one, shift_one = norm_backward(
        act_one_grad * swish_slope(pre_one), normed_one, inverse_one, norm_gains[0], members
    )
    input_grad = residual_grad + input_back
    conv_grad = jnp.stack([weight_one_grad, weight_two_grad])
    conv_part = lax.psum_scatter(conv_grad, "height", scatter_dimension=4, tiled=True)
    conv_part = lax.psum_scatter(
        conv_part.astype(jnp.bfloat16), "canvas", scatter_dimension=3, tiled=True
    ).astype(jnp.float32)
    summed = lax.psum(
        (
            jnp.stack([gain_one, gain_two, gain_three]),
            jnp.stack([shift_one, shift_two, shift_three]),
            jnp.stack([bias_one_grad, bias_two_grad]),
            qkv_grad,
            qv_grad,
            proj_grad,
            proj_bias_grad,
        ),
        ("canvas", "height"),
    )
    return (
        output.astype(jnp.bfloat16).reshape((1,) + grid_shape),
        input_grad.astype(jnp.bfloat16).reshape((1,) + grid_shape),
        summed[0],
        summed[1],
        conv_part,
        summed[2],
        summed[3],
        summed[4],
        summed[5],
        summed[6],
    )


def fold(block):
    rows, width = block.shape
    return jnp.sum(block.reshape(rows // 8, 8, width), axis=0)


def group_lanes(block, group):
    lane = lax.broadcasted_iota(jnp.int32, block.shape, 1)
    width = block.shape[1]
    step = 1
    while step < group:
        above = pltpu.roll(block, step, 1)
        below = pltpu.roll(block, width - step, 1)
        block = block + jnp.where((lane & step) != 0, above, below)
        step *= 2
    return block


def group_mean(partial, members):
    spread = group_lanes(partial, partial.shape[1] // GROUPS)
    return jnp.sum(spread, axis=0, keepdims=True) * (1.0 / members)


def widen(block, width):
    return jnp.concatenate([block] * (width // block.shape[1]), axis=1)


def each_block(pixels, block, body, carry=0):
    def step(index, carry):
        return body(pl.ds(pl.multiple_of(index * block, block), block), carry)

    return lax.fori_loop(0, pixels // block, step, carry)


def each_chunk(pixels, body, carry):
    return each_block(pixels, CHUNK, body, carry)


def aligned(start, step):
    return start if isinstance(start, int) else pl.multiple_of(start, step)


class RunningStats:
    def __init__(self, channels):
        self.width = channels // GROUPS
        self.reference = None
        self.sums = self.squares = jnp.zeros((8, channels), jnp.float32)

    def add(self, block):
        if self.reference is None:
            self.reference = group_mean(block[0:8], 8.0 * self.width)
        offset = block - self.reference
        self.sums = self.sums + fold(offset)
        self.squares = self.squares + fold(offset * offset)

    def finish(self, pixels):
        both = group_lanes(jnp.concatenate([self.sums, self.squares], axis=0), self.width)
        share = 1.0 / (pixels * self.width)
        offset = column_total(both[0:8]) * share
        variance = column_total(both[8:16]) * share - offset * offset
        return self.reference + offset, lax.rsqrt(jnp.maximum(variance, 0.0) + epsilon)


def put_taps(taps_ref, block, rows, cols):
    count, channels = block.shape
    place = lax.broadcasted_iota(jnp.int32, block.shape, 0) & (cols - 1)
    left = jnp.where(place == 0, 0.0, pltpu.roll(block, 1, 0))
    right = jnp.where(place == cols - 1, 0.0, pltpu.roll(block, count - 1, 0))
    inner = pl.ds(aligned(rows.start + cols, cols), count)
    taps_ref[inner, 0:channels] = left.astype(jnp.bfloat16)
    taps_ref[inner, channels : 2 * channels] = block.astype(jnp.bfloat16)
    taps_ref[inner, 2 * channels :] = right.astype(jnp.bfloat16)


def clear_edges(taps_ref, cols):
    edge = jnp.zeros((cols, taps_ref.shape[1]), taps_ref.dtype)
    taps_ref[0:cols, :] = edge
    taps_ref[taps_ref.shape[0] - cols :, :] = edge


def begin_conv(taps_ref, product, total_ref, fill, first, cols):
    for start in range(0, total_ref.shape[0], FILL_ROWS):
        for inner in range(start, start + FILL_ROWS, CHUNK):
            fill(pl.ds(inner, CHUNK))
        rows = pl.ds(start, FILL_ROWS)
        total_ref[rows, :] = first(rows, product(taps_ref, pl.ds(start + cols, FILL_ROWS), 1))


def add_rows(taps_ref, product, mask_ref, total_ref, row_tap, last, cols, old_ref=None):
    pixels, channels = total_ref.shape
    old_ref = total_ref if old_ref is None else old_ref
    for start in range(0, pixels, FILL_ROWS):
        rows = slice(start, start + FILL_ROWS)
        part = product(taps_ref, pl.ds(start + row_tap * cols, FILL_ROWS), row_tap)
        mask = widen(mask_ref[row_tap // 2, rows, :], channels)
        total_ref[rows, :] = last(rows, old_ref[rows, :] + mask * part)


def run_conv(taps_ref, product, mask_ref, total_ref, fill, first, last, cols):
    begin_conv(taps_ref, product, total_ref, fill, first, cols)
    add_rows(taps_ref, product, mask_ref, total_ref, 0, lambda rows, value: value, cols)
    add_rows(taps_ref, product, mask_ref, total_ref, 2, last, cols)


def product_forward(weight_ref):
    channels = weight_ref.shape[-1]

    def product(taps_ref, shifted, row_tap):
        return jnp.dot(
            taps_ref[shifted, :],
            weight_ref[row_tap].reshape(3 * channels, channels),
            preferred_element_type=jnp.float32,
        )

    return product


def product_backward(weight_ref):
    def product(taps_ref, shifted, row_tap):
        return lax.dot_general(
            taps_ref[shifted, :],
            weight_ref[row_tap],
            (((1,), (1,)), ((), ())),
            preferred_element_type=jnp.float32,
        )

    return product


def activation(read, mean, inverse, gain, shift, act_ref, taps_ref, cols):
    scale, offset = 0.5 * inverse * gain, 0.5 * shift

    def fill(rows):
        half = (read(rows) - mean) * scale + offset
        act = half * (1.0 + jnp.tanh(half))
        act_ref[rows, :] = act.astype(jnp.bfloat16)
        put_taps(taps_ref, act, rows, cols)

    return fill


def back_means(sums, gain, pixels):
    channels = gain.shape[1]
    members = float(pixels * (channels // GROUPS))
    return group_mean(sums[0] * gain, members), group_mean(sums[1] * gain, members)


def column_total(partial):
    return jnp.sum(partial, axis=0, keepdims=True)


def weight_part(act_ref, narrow, lanes_ref, flip_ref, columns_ref, part_ref, cols):
    pixels, channels = act_ref.shape
    height = lax.axis_index("height")
    share = NARROW // 2
    flip_ref[...] = narrow.T
    own = pl.ds(pl.multiple_of((height % 2) * share, share), share)
    grad = flip_ref[own, :].astype(jnp.float32)
    column = lax.broadcasted_iota(jnp.int32, grad.shape, 1) & (cols - 1)
    for col_tap in range(3):
        shifted = grad
        if col_tap == 0:
            shifted = jnp.where(column == cols - 1, 0.0, pltpu.roll(grad, pixels - 1, 1))
        elif col_tap == 2:
            shifted = jnp.where(column == 0, 0.0, pltpu.roll(grad, 1, 1))
        for row_tap in range(3):
            tap = 3 * row_tap + col_tap
            place = slice(tap * share, (tap + 1) * share)
            if row_tap == 1:
                columns_ref[place, :] = shifted.astype(jnp.bfloat16)
                continue
            side, turn = (0, pixels - cols) if row_tap == 0 else (1, cols)
            masked = (shifted * lanes_ref[side : side + 1, :]).astype(jnp.bfloat16)
            columns_ref[place, :] = pltpu.roll(masked, turn, 1)
    part_ref[...] = jnp.dot(
        columns_ref[...], act_ref[...], preferred_element_type=jnp.float32
    ).astype(jnp.bfloat16)


def begin_back(grad_ref, weights_ref, mask_ref, taps_ref, total_ref, cols):
    clear_edges(taps_ref, cols)

    def fill(rows):
        put_taps(taps_ref, grad_ref[rows, :].astype(jnp.float32), rows, cols)

    product = product_backward(weights_ref)
    begin_conv(taps_ref, product, total_ref, fill, lambda rows, part: part, cols)
    add_rows(taps_ref, product, mask_ref, total_ref, 0, lambda rows, value: value, cols)


def finish_back(
    weights_ref, mask_ref, taps_ref, total_ref, read, table_ref, which, cols, old_ref=None
):
    mean, inverse, gain, shift = norm_rows(table_ref, which)
    scale, offset = 0.5 * inverse * gain, 0.5 * shift
    sums = []

    def slope(rows, value):
        centered = read(rows) - mean
        half = centered * scale + offset
        turn = jnp.tanh(half)
        double = value * ((1.0 + turn) * (1.0 + half * (1.0 - turn)))
        sums.append((fold(double), fold(double * centered)))
        return double

    add_rows(
        taps_ref, product_backward(weights_ref), mask_ref, total_ref, 2, slope, cols, old_ref
    )
    plain, cross = sum(pair[0] for pair in sums), sum(pair[1] for pair in sums)
    return 0.5 * plain, 0.5 * inverse * cross


def norm_back(total_ref, double, sums, read, table_ref, which, pixels, scales_ref=None):
    mean, inverse, gain, shift = norm_rows(table_ref, which)
    mean_grad, mean_cross = back_means(sums, gain, pixels)
    slope = inverse * gain * (0.5 if double else 1.0)
    level, tilt = inverse * mean_grad, inverse * inverse * mean_cross
    if scales_ref is not None:
        for row, scales in enumerate((mean, slope, level, tilt)):
            scales_ref[row : row + 1, :] = scales

    def back(rows, inner):
        return total_ref[inner, :] * slope - level - (read(rows) - mean) * tilt

    return back


def own_lanes():
    block = lax.axis_index("height") // 2
    return pl.ds(pl.multiple_of(block * NARROW, NARROW), NARROW)


def narrow_back(total_ref, value_ref, scales_ref):
    lanes = own_lanes()
    mean, slope, level, tilt = (scales_ref[row : row + 1, lanes] for row in range(4))
    return total_ref[:, lanes] * slope - level - (value_ref[:, lanes] - mean) * tilt


def turn_kernel(
    grad_ref, mask_ref, weights_ref, middle_ref, table_ref, total_ref, sums_ref, taps_ref, *, cols
):
    begin_back(grad_ref, weights_ref.at[1], mask_ref, taps_ref, total_ref, cols)
    sums_ref[0:8, :], sums_ref[8:16, :] = finish_back(
        weights_ref.at[1],
        mask_ref,
        taps_ref,
        total_ref,
        lambda rows: middle_ref[rows, :],
        table_ref,
        1,
        cols,
    )


def norm_rows(table_ref, which):
    picks = (2 * which, 2 * which + 1, 6 + which, 9 + which)
    return tuple(table_ref[pick : pick + 1, :] for pick in picks)


def build_masks(ids_ref, mask_ref, lanes_ref, id_rows_ref, id_cols_ref, cols):
    rows = ids_ref.shape[1]
    for row in range(rows):
        here = ids_ref[0, row]
        place = slice(row * cols, (row + 1) * cols)
        id_rows_ref[place, :] = jnp.full((cols, LANES), here, jnp.int32)
        for side, other in ((0, row - 1), (1, row + 1)):
            same = jnp.float32(0.0)
            if 0 <= other < rows:
                same = jnp.where(ids_ref[0, other] == here, 1.0, 0.0).astype(jnp.float32)
            mask_ref[side, place, :] = jnp.full((cols, LANES), same, jnp.float32)
    lane = lax.broadcasted_iota(jnp.int32, (8, LANES), 1)
    each = LANES // cols
    for block in range(rows // each):
        ids = jnp.full((8, LANES), ids_ref[0, block * each], jnp.int32)
        for step in range(1, each):
            ids = jnp.where(lane >= step * cols, ids_ref[0, block * each + step], ids)
        id_cols_ref[:, block * LANES : (block + 1) * LANES] = ids
    ids = id_cols_ref[...].astype(jnp.float32)
    pixels = ids.shape[1]
    pixel = lax.broadcasted_iota(jnp.int32, ids.shape, 1)
    above = jnp.where(pixel < cols, -1.0, pltpu.roll(ids, cols, 1))
    below = jnp.where(pixel >= pixels - cols, -1.0, pltpu.roll(ids, pixels - cols, 1))
    lanes_ref[0:1, :] = jnp.where(above == ids, 1.0, 0.0)[0:1]
    lanes_ref[1:2, :] = jnp.where(below == ids, 1.0, 0.0)[0:1]


def place_pieces(pieces, whole_ref, sems):
    own_pixels = whole_ref.shape[0] // len(pieces)
    height = lax.axis_index("height")
    copies = []
    for place, piece in enumerate(pieces):
        start = pl.multiple_of((height ^ place) * own_pixels, own_pixels)
        rows = pl.ds(start, own_pixels)
        copies.append(pltpu.make_async_copy(piece, whole_ref.at[rows, :], sems.at[place]))
    return copies


def hold_kernel(
    ids_hbm,
    gains_hbm,
    shifts_hbm,
    biases_hbm,
    weights_hbm,
    qkv_hbm,
    proj_hbm,
    qv_bias_hbm,
    proj_bias_hbm,
    weights_ref,
    turned_ref,
    qkv_ref,
    proj_ref,
    table_ref,
    mask_ref,
    lanes_ref,
    id_rows_ref,
    id_cols_ref,
    ids_ref,
    gains_ref,
    shifts_ref,
    biases_ref,
    qv_bias_ref,
    proj_bias_ref,
    sems,
    *,
    cols,
):
    channels = weights_ref.shape[-1]
    small = [
        (ids_hbm, ids_ref),
        (gains_hbm, gains_ref),
        (shifts_hbm, shifts_ref),
        (biases_hbm, biases_ref),
        (qv_bias_hbm, qv_bias_ref),
        (proj_bias_hbm, proj_bias_ref),
    ]
    large = [(weights_hbm, weights_ref), (qkv_hbm, qkv_ref), (proj_hbm, proj_ref)]
    for which in range(2):
        for row_tap in range(3):
            for col_tap in range(3):
                place = slice(col_tap * channels, (col_tap + 1) * channels)
                large.append(
                    (
                        weights_hbm.at[which, 2 - row_tap, 2 - col_tap],
                        turned_ref.at[which, row_tap, :, place],
                    )
                )
    copies = [
        pltpu.make_async_copy(source, target, sems.at[index])
        for index, (source, target) in enumerate(small + large)
    ]
    for copy in copies:
        copy.start()
    for copy in copies[: len(small)]:
        copy.wait()
    build_masks(ids_ref, mask_ref, lanes_ref, id_rows_ref, id_cols_ref, cols)
    table_ref[6:9, :] = gains_ref[...]
    table_ref[9:12, :] = shifts_ref[...]
    table_ref[12:14, :] = biases_ref[...]
    table_ref[14:16, :] = qv_bias_ref[...]
    table_ref[16:17, :] = proj_bias_ref[...]
    for copy in copies[len(small) :]:
        copy.wait()


def conv_kernel(*refs, cols, count):
    pieces, refs = refs[:count], refs[count:]
    (
        weights_ref,
        params_ref,
        mask_ref,
        features_ref,
        act_one_ref,
        middle_ref,
        act_two_ref,
        residual_ref,
        table_ref,
        own_ref,
        taps_ref,
        sem,
    ) = refs
    pixels, channels = features_ref.shape
    wide = jnp.float32
    own_copy = pltpu.make_async_copy(pieces[0], own_ref, sem)
    own_copy.start()
    table_ref[...] = params_ref[...]
    clear_edges(taps_ref, cols)

    def read_input(rows):
        return features_ref[rows, :].astype(wide)

    def read_middle(rows):
        return middle_ref[rows, :]

    height = lax.axis_index("height")
    own_pixels = pixels // count
    seen = RunningStats(channels)
    for place in list(range(1, count)) + [0]:
        if place == 0:
            own_copy.wait()
        piece = (pieces[place] if place else own_ref)[...]
        start = pl.multiple_of((height ^ place) * own_pixels, own_pixels)
        features_ref[pl.ds(start, own_pixels), :] = piece
        seen.add(piece.astype(wide))
    table_ref[0:1, :], table_ref[1:2, :] = seen.finish(pixels)
    seen = RunningStats(channels)

    def keep(rows, value):
        seen.add(value)
        return value

    run_conv(
        taps_ref,
        product_forward(weights_ref.at[0]),
        mask_ref,
        middle_ref,
        activation(read_input, *norm_rows(table_ref, 0), act_one_ref, taps_ref, cols),
        lambda rows, part: part + table_ref[12:13, :],
        keep,
        cols,
    )
    table_ref[2:3, :], table_ref[3:4, :] = seen.finish(pixels)
    seen = RunningStats(channels)
    run_conv(
        taps_ref,
        product_forward(weights_ref.at[1]),
        mask_ref,
        residual_ref,
        activation(read_middle, *norm_rows(table_ref, 1), act_two_ref, taps_ref, cols),
        lambda rows, part: part + (read_input(rows) + table_ref[13:14, :]),
        keep,
        cols,
    )
    table_ref[4:5, :], table_ref[5:6, :] = seen.finish(pixels)


def score_kernel(
    qkv_ref,
    proj_ref,
    residual_ref,
    table_ref,
    id_rows_ref,
    id_cols_ref,
    normed_ref,
    query_ref,
    key_ref,
    value_ref,
    soft_ref,
    out_flip_ref,
    output_ref,
    value_flip_ref,
    *scores_refs,
    score_scale,
):
    pixels, channels = residual_ref.shape
    own_pixels = output_ref.shape[0]
    wide = jnp.float32
    exponent = score_scale * 1.4426950408889634
    mean, inverse, gain, shift = norm_rows(table_ref, 2)
    scale = inverse * gain

    def normalise(start):
        rows = slice(start, start + KEY_ROWS)
        normed = (residual_ref[rows, :] - mean) * scale + shift
        normed_ref[rows, :] = normed.astype(jnp.bfloat16)

    def project(start):
        rows = slice(start, start + KEY_ROWS)
        normed = normed_ref[rows, :]
        query_ref[rows, :] = (
            jnp.dot(normed, qkv_ref[:, 0:channels], preferred_element_type=wide)
            + table_ref[14:15, :]
        ).astype(jnp.bfloat16)
        key_ref[rows, :] = jnp.dot(
            normed, qkv_ref[:, channels : 2 * channels], preferred_element_type=wide
        ).astype(jnp.bfloat16)
        values = (
            jnp.dot(normed, qkv_ref[:, 2 * channels :], preferred_element_type=wide)
            + table_ref[15:16, :]
        ).astype(jnp.bfloat16)
        value_ref[rows, :] = values
        value_flip_ref[:, rows] = values.T

    normalise(0)
    for start in range(0, pixels, KEY_ROWS):
        if start + KEY_ROWS < pixels:
            normalise(start + KEY_ROWS)
        project(start)
    block = scores_refs[0].shape[1]
    steps = range(0, pixels, KEY_ROWS)

    def score(index):
        rows = slice(index * block, (index + 1) * block)
        for start in steps:
            keys = slice(start, start + KEY_ROWS)
            scores = lax.dot_general(
                key_ref[keys, :],
                query_ref[rows, :],
                (((1,), (1,)), ((), ())),
                preferred_element_type=wide,
            )
            same = widen(id_rows_ref[keys, :], block) == id_cols_ref[0:1, rows]
            scores_refs[index][keys, :] = jnp.where(same, scores, masked_score)

    def soften(index):
        rows = slice(index * block, (index + 1) * block)
        scores_ref = scores_refs[index]
        peak = jnp.full((8, block), masked_score, wide)
        for start in steps:
            scores = scores_ref[start : start + KEY_ROWS, :]
            peak = jnp.maximum(peak, jnp.max(scores.reshape(-1, 8, block), axis=0))
        peak = jnp.max(peak, axis=0, keepdims=True)
        total = jnp.zeros((8, block), wide)
        for start in steps:
            keys = slice(start, start + KEY_ROWS)
            powers = jnp.exp2((scores_ref[keys, :] - peak) * exponent)
            scores_ref[keys, :] = powers
            total = total + fold(powers)
        share = 1.0 / column_total(total)
        for start in steps:
            keys = slice(start, start + KEY_ROWS)
            soft_ref[keys, rows] = (scores_ref[keys, :] * share).astype(jnp.bfloat16)

    score(0)
    for index in range(len(scores_refs)):
        if index + 1 < len(scores_refs):
            score(index + 1)
        soften(index)

    def collect(rows, carry):
        out_flip_ref[rows, :] = jnp.dot(
            value_flip_ref[rows, :], soft_ref[...], preferred_element_type=wide
        ).astype(jnp.bfloat16)
        return carry

    each_block(channels, channels // 2, collect)
    height = lax.axis_index("height")
    own = pl.ds(pl.multiple_of(height * own_pixels, own_pixels), own_pixels)
    output_ref[...] = (
        residual_ref[own, :]
        + lax.dot_general(
            out_flip_ref[:, own],
            proj_ref[...],
            (((0,), (0,)), ((), ())),
            preferred_element_type=wide,
        )
        + table_ref[16:17, :]
    ).astype(jnp.bfloat16)


def own_quarter():
    height = lax.axis_index("height")
    return (height & 1) * 2 + ((height >> 1) & 1)


def send_order(source_ref, targets, axis, share):
    me = lax.axis_index("canvas")
    for step, target in enumerate(targets):
        place = pl.ds(pl.multiple_of((me ^ step) * share, share), share)
        target[...] = source_ref[place, :] if axis == 0 else source_ref[:, place]


def attention_kernel(
    proj_ref,
    normed_ref,
    query_ref,
    key_ref,
    value_ref,
    soft_ref,
    out_flip_ref,
    *refs,
    score_scale,
    count,
):
    pieces, (grad_ref, packed_ref, sums_ref), refs = (
        refs[:count],
        refs[count : count + 3],
        refs[count + 3 :],
    )
    pixels, channels = normed_ref.shape
    blocks = pixels // SCORE_ROWS
    grads_refs, refs = refs[-blocks:], refs[:-blocks]
    *mixed_refs, mixed_ref, key_flip_ref, back_ref, score_grad_ref, flip_ref, sems = refs
    wide = jnp.float32
    copies = place_pieces(pieces, grad_ref, sems)
    for copy in copies:
        copy.start()
    quarter = channels // 4
    own = pl.ds(pl.multiple_of(own_quarter() * quarter, quarter), quarter)
    flip_ref[...] = normed_ref[:, own].T
    key_flip_ref[...] = key_ref[...].T
    for copy in copies:
        copy.wait()
    block, count = SCORE_ROWS, blocks
    steps = range(0, pixels, KEY_ROWS)

    def block_rows(index):
        return slice(index * block, (index + 1) * block)

    for index in range(count):
        back_ref[block_rows(index), :] = lax.dot_general(
            grad_ref[block_rows(index), :],
            proj_ref[...],
            (((1,), (1,)), ((), ())),
            preferred_element_type=wide,
        ).astype(jnp.bfloat16)

    def weigh(index):
        total = jnp.zeros((8, block), wide)
        for start in steps:
            keys = slice(start, start + KEY_ROWS)
            weight_grad = lax.dot_general(
                value_ref[keys, :],
                back_ref[block_rows(index), :],
                (((1,), (1,)), ((), ())),
                preferred_element_type=wide,
            )
            grads_refs[index][keys, :] = weight_grad
            total = total + fold(soft_ref[keys, block_rows(index)].astype(wide) * weight_grad)
        return column_total(total)

    def slope(index, dots):
        for start in steps:
            keys = slice(start, start + KEY_ROWS)
            weights = soft_ref[keys, block_rows(index)].astype(wide)
            score_grad_ref[keys, block_rows(index)] = (
                weights * (grads_refs[index][keys, :] - dots)
            ).astype(jnp.bfloat16)

    dots = weigh(0)
    for index in range(count):
        now, rows = dots, block_rows(index)
        if index + 1 < count:
            dots = weigh(index + 1)
        slope(index, now)
        packed_ref[rows, 2 * channels :] = jnp.dot(
            soft_ref[rows, :], back_ref[...], preferred_element_type=wide
        ).astype(jnp.bfloat16)
        query_grad = jnp.dot(
            key_flip_ref[...], score_grad_ref[:, rows], preferred_element_type=wide
        )
        packed_ref[rows, 0:channels] = (query_grad * score_scale).astype(jnp.bfloat16).T
    for index in range(count):
        rows = block_rows(index)
        packed_ref[rows, channels : 2 * channels] = (
            jnp.dot(score_grad_ref[rows, :], query_ref[...], preferred_element_type=wide)
            * score_scale
        ).astype(jnp.bfloat16)

    def pack(rows, carry):
        return (
            carry[0] + fold(packed_ref[rows, 0:channels].astype(wide)),
            carry[1] + fold(packed_ref[rows, 2 * channels :].astype(wide)),
            carry[2] + fold(grad_ref[rows, :].astype(wide)),
        )

    zeros = jnp.zeros((8, channels), wide)
    totals = zeros, zeros, zeros
    for start in range(0, pixels, CHUNK):
        totals = pack(pl.ds(start, CHUNK), totals)
    sums_ref[...] = jnp.zeros(sums_ref.shape, wide)
    for row, total in enumerate(totals):
        sums_ref[8 + row : 9 + row, :] = column_total(total)
    mixed_ref[:, 0 : 3 * channels] = jnp.dot(
        flip_ref[...], packed_ref[...], preferred_element_type=wide
    ).astype(jnp.bfloat16)
    mixed_ref[:, 3 * channels :] = jnp.dot(
        out_flip_ref[own, :], grad_ref[...], preferred_element_type=wide
    ).astype(jnp.bfloat16)
    send_order(mixed_ref, mixed_refs, 0, quarter // len(mixed_refs))


def third_kernel(
    qkv_ref,
    grad_ref,
    packed_ref,
    residual_ref,
    table_ref,
    act_two_ref,
    lanes_ref,
    old_sums_ref,
    residual_grad_ref,
    grad_two_ref,
    sums_ref,
    keep_ref,
    send_ref,
    total_ref,
    flip_ref,
    columns_ref,
    part_ref,
    scales_ref,
    *,
    cols,
):
    pixels, channels = residual_ref.shape
    block = FILL_ROWS
    wide = jnp.float32
    mean, inverse, gain, shift = norm_rows(table_ref, 2)
    zeros = jnp.zeros((8, channels), wide)

    sums = (zeros, zeros)
    for start in range(0, pixels, block):
        rows = pl.ds(start, block)
        normed_grad = lax.dot_general(
            packed_ref[rows, :], qkv_ref[...], (((1,), (1,)), ((), ())), preferred_element_type=wide
        )
        total_ref[rows, :] = normed_grad
        centered = residual_ref[rows, :] - mean
        sums = sums[0] + fold(normed_grad), sums[1] + fold(normed_grad * centered)
    sums = sums[0], sums[1] * inverse
    sums_ref[...] = old_sums_ref[...]
    sums_ref[5:6, :] = column_total(sums[1])
    sums_ref[6:7, :] = column_total(sums[0])
    back = norm_back(
        total_ref, False, sums, lambda rows: residual_ref[rows, :], table_ref, 2, pixels, scales_ref
    )
    narrow = narrow_back(total_ref, residual_ref, scales_ref)
    narrow = (grad_ref[:, own_lanes()].astype(wide) + narrow).astype(jnp.bfloat16)
    weight_part(act_two_ref, narrow, lanes_ref, flip_ref, columns_ref, part_ref, cols)

    def finish(rows, carry):
        total = grad_ref[rows, :].astype(wide) + back(rows, rows)
        residual_grad_ref[rows, :] = total
        low = total.astype(jnp.bfloat16)
        grad_two_ref[rows, :] = low
        return carry + fold(low.astype(wide))

    total = zeros
    for start in range(0, pixels, CHUNK):
        total = finish(pl.ds(start, CHUNK), total)
    sums_ref[7:8, :] = column_total(total)
    keep_half(part_ref, 2, 1, keep_ref, send_ref)


def second_kernel(
    total_ref,
    partial_ref,
    middle_ref,
    table_ref,
    act_one_ref,
    lanes_ref,
    old_sums_ref,
    grad_one_ref,
    sums_ref,
    keep_ref,
    send_ref,
    flip_ref,
    columns_ref,
    part_ref,
    scales_ref,
    *,
    cols,
):
    pixels, channels = middle_ref.shape
    sums = partial_ref[0:8, :], partial_ref[8:16, :]
    back = norm_back(
        total_ref, True, sums, lambda rows: middle_ref[rows, :], table_ref, 1, pixels, scales_ref
    )
    narrow = narrow_back(total_ref, middle_ref, scales_ref).astype(jnp.bfloat16)
    weight_part(act_one_ref, narrow, lanes_ref, flip_ref, columns_ref, part_ref, cols)
    sums_ref[...] = old_sums_ref[...]
    sums_ref[2:3, :] = column_total(sums[1])
    sums_ref[3:4, :] = column_total(sums[0])

    def finish(rows, carry):
        low = back(rows, rows).astype(jnp.bfloat16)
        grad_one_ref[rows, :] = low
        return carry + fold(low.astype(jnp.float32))

    zeros = jnp.zeros((8, channels), jnp.float32)
    total = zeros
    for start in range(0, pixels, CHUNK):
        total = finish(pl.ds(start, CHUNK), total)
    sums_ref[4:5, :] = column_total(total)
    keep_half(part_ref, 1, 2, keep_ref, send_ref)


def keep_half(part_ref, near, far, keep_ref, send_ref):
    me = lax.axis_index("canvas")
    rows, width = part_ref.shape[0], keep_ref.shape[1]
    for target_ref, flip in ((keep_ref, 0), (send_ref, near)):
        for slot in range(2):
            owner = me ^ flip ^ (slot * far)
            place = pl.ds(pl.multiple_of(owner * width, width), width)
            target_ref[slot * rows : (slot + 1) * rows, :] = part_ref[:, place]


def first_kernel(
    grad_one_ref,
    features_ref,
    table_ref,
    mask_ref,
    old_sums_ref,
    weights_ref,
    own_ref,
    sums_ref,
    partial_ref,
    total_ref,
    taps_ref,
    *,
    cols,
):
    def read(rows):
        return features_ref[rows, :].astype(jnp.float32)

    weights = weights_ref.at[0]
    begin_back(grad_one_ref, weights, mask_ref, taps_ref, total_ref, cols)
    sums = finish_back(weights, mask_ref, taps_ref, total_ref, read, table_ref, 0, cols)
    partial_ref[0:8, :], partial_ref[8:16, :] = sums
    sums_ref[...] = old_sums_ref[...]
    sums_ref[0:1, :] = column_total(sums[1])
    sums_ref[1:2, :] = column_total(sums[0])
    count = own_ref.shape[0]
    own = pl.ds(pl.multiple_of(lax.axis_index("height") * count, count), count)
    own_ref[...] = total_ref[own, :]


def own_kernel(
    own_ref, partial_ref, features_ref, residual_grad_ref, table_ref, input_grad_ref
):
    def read(rows):
        return features_ref[rows, :].astype(jnp.float32)

    sums = partial_ref[0:8, :], partial_ref[8:16, :]
    pixels = features_ref.shape[0]
    back = norm_back(own_ref, True, sums, read, table_ref, 0, pixels)
    count = own_ref.shape[0]
    own = pl.ds(pl.multiple_of(lax.axis_index("height") * count, count), count)
    total = residual_grad_ref[own, :] + back(own, slice(0, count))
    input_grad_ref[...] = total.astype(jnp.bfloat16)


def place_kernel(*refs):
    joints, packed_ref = refs[:-1], refs[-1]
    share = packed_ref.shape[0] // len(joints)
    me = lax.axis_index("canvas")
    for step, joint in enumerate(joints):
        place = pl.ds(pl.multiple_of((me ^ step) * share, share), share)
        packed_ref[place, :] = joint[...]


def spread_quarters(packed, flips, qkv_ref, proj_ref, qkv_hbm, proj_hbm, sems):
    quarter = packed[0].shape[0]
    inner = qkv_ref.shape[2]
    copies = []
    for index, packed_ref in enumerate(packed):
        owner = own_quarter() ^ flips[index]
        rows = pl.ds(pl.multiple_of(owner * quarter, quarter), quarter)
        qkv_ref[index] = packed_ref[:, 0:inner].astype(jnp.float32)
        proj_ref[index] = packed_ref[:, inner:].astype(jnp.float32)
        for which, (held, target) in enumerate(((qkv_ref, qkv_hbm), (proj_ref, proj_hbm))):
            copy = pltpu.make_async_copy(held.at[index], target.at[rows, :], sems.at[index, which])
            copy.start()
            copies.append(copy)
    return copies


def join_kernel(*refs):
    packed, (qkv_hbm, proj_hbm, qkv_ref, proj_ref, sems) = refs[:-5], refs[-5:]
    copies = spread_quarters(
        packed, range(len(packed)), qkv_ref, proj_ref, qkv_hbm, proj_hbm, sems
    )
    for copy in copies:
        copy.wait()


def halve_kernel(keep_ref, got_ref, hold_ref, send_ref):
    total = keep_ref[...].astype(jnp.float32) + got_ref[...].astype(jnp.float32)
    rows = hold_ref.shape[0]
    hold_ref[...] = total[0:rows]
    send_ref[0:rows, :] = total[rows:].astype(jnp.bfloat16)


def halve_sums_kernel(
    keep_one_ref,
    got_one_ref,
    keep_two_ref,
    got_two_ref,
    sums_ref,
    hold_ref,
    send_ref,
    hold_two_ref,
    send_two_ref,
):
    halve_kernel(keep_one_ref, got_one_ref, hold_ref, send_ref)
    halve_kernel(keep_two_ref, got_two_ref, hold_two_ref, send_two_ref)
    rows = hold_ref.shape[0]
    left = sums_ref[...]
    count, width = left.shape
    for part in range(2):
        low = left.astype(jnp.bfloat16)
        left = left - low.astype(jnp.float32)
        for block in range(width // LANES):
            send_ref[rows : rows + count, :] = low[:, block * LANES : (block + 1) * LANES]
            rows += count


def unpack_sums(got_ref, rows, count, width):
    total = jnp.zeros((count, width), jnp.float32)
    for part in range(2):
        blocks = []
        for block in range(width // LANES):
            blocks.append(got_ref[rows : rows + count, :].astype(jnp.float32))
            rows += count
        total = total + jnp.concatenate(blocks, axis=1)
    return total


def sums_kernel(
    sums_ref,
    near_ref,
    far_ref,
    hold_one_ref,
    got_one_ref,
    hold_two_ref,
    got_two_ref,
    share_ref,
    gains_ref,
    shifts_ref,
    conv_ref,
    qv_ref,
    bias_ref,
):
    rows = hold_one_ref.shape[0]
    for which, (hold_ref, got_ref) in enumerate(
        ((hold_one_ref, got_one_ref), (hold_two_ref, got_two_ref))
    ):
        total = hold_ref[...] + got_ref[0:rows, :].astype(jnp.float32)
        share_ref[which] = total.reshape(share_ref.shape[1:])
    total = sums_ref[...] + near_ref[...] + far_ref[...]
    total = total + unpack_sums(got_one_ref, rows, *total.shape)
    for row, start in enumerate((0, 2, 5)):
        gains_ref[row : row + 1, :] = total[start : start + 1]
        shifts_ref[row : row + 1, :] = total[start + 1 : start + 2]
    conv_ref[0:1, :] = total[4:5]
    conv_ref[1:2, :] = total[7:8]
    qv_ref[...] = total[8:10]
    bias_ref[...] = total[10:11]


def call_kernel(kernel, outputs, scratch, operands, places, flops, limit, out_places=None, aliases={}):
    out_places = out_places or "v" * len(outputs)
    spaces = {
        "v": pl.BlockSpec(memory_space=pltpu.VMEM),
        "s": pl.BlockSpec(memory_space=pltpu.SMEM),
        "h": pl.BlockSpec(memory_space=pl.ANY),
        "o": pl.BlockSpec(memory_space=pltpu.VMEM),
        "a": pl.BlockSpec(memory_space=pl.ANY),
    }
    moved = 8 * flops // LANES
    held = {"v": pltpu.VMEM, "h": pltpu.HBM, "o": jax.ShapeDtypeStruct}
    operands = [
        pltpu.with_memory_space_constraint(array, pltpu.HBM) if place == "h" else array
        for array, place in zip(operands, places)
    ]
    return pl.pallas_call(
        kernel,
        out_shape=[held[place](*output) for output, place in zip(outputs, out_places)],
        in_specs=[spaces[place] for place in places],
        out_specs=[spaces[place] for place in out_places],
        scratch_shapes=scratch,
        input_output_aliases=aliases,
        compiler_params=pltpu.CompilerParams(vmem_limit_bytes=limit * 2**20),
        cost_estimate=pl.CostEstimate(flops=flops, bytes_accessed=moved, transcendentals=0),
    )(*operands)


def send_height(block, step):
    size = lax.axis_size("height")
    return lax.ppermute(block, "height", [(i, i ^ step) for i in range(size)])


def with_cores(blocks):
    return [piece for block in blocks for piece in (block, send_height(block, 1))]


def send_canvas(block, step):
    size = lax.axis_size("canvas")
    return lax.ppermute(block, "canvas", [(i, i ^ step) for i in range(size)])


def trade_canvas(pieces):
    return [pieces[0]] + [send_canvas(piece, step) for step, piece in enumerate(pieces) if step]


def whole_canvas(
    features,
    tile_ids,
    norm_gains,
    norm_shifts,
    conv_weights,
    conv_biases,
    qkv_weight,
    qv_bias,
    proj_weight,
    proj_bias,
    cotangent,
):
    height_size = lax.axis_size("height")
    canvas_size = lax.axis_size("canvas")
    local_rows, cols, channels = features.shape[1:]
    all_rows = tile_ids.shape[1]
    pixels = all_rows * cols
    own_pixels = local_rows * cols
    out_share = channels // height_size
    ci_share = channels // canvas_size
    quarter = channels // 4
    row_share = quarter // canvas_size
    low, wide = jnp.bfloat16, jnp.float32

    own_features = features.reshape(own_pixels, channels)
    own_grad = cotangent.reshape(own_pixels, channels)
    steps = range(2, height_size, 2)
    held_features = [own_features] + [send_height(own_features, step) for step in steps]
    plane = ((pixels, channels), low)
    plane_wide = ((pixels, channels), wide)
    sums_shape = ((16, channels), wide)
    mixed_shapes = [((row_share, 4 * channels), low)] * canvas_size
    taps = pltpu.VMEM((pixels + 2 * cols, 3 * channels), low)
    held_wide = pltpu.VMEM((pixels, channels), wide)
    flipped = pltpu.VMEM((channels, pixels), low)
    narrow = pltpu.VMEM((NARROW, pixels), low)
    columns = pltpu.VMEM((9 * out_share, pixels), low)
    part_held = pltpu.VMEM((9 * out_share, channels), low)
    sem = pltpu.SemaphoreType.DMA
    conv_flops = 2 * 9 * pixels * channels * channels
    dot_flops = 2 * pixels * channels * channels
    score_flops = 2 * pixels * pixels * channels
    scale = channels ** (-0.5)

    (
        held_conv,
        turned,
        held_qkv,
        held_proj,
        params,
        mask,
        lane_mask,
        id_rows,
        id_cols,
    ) = call_kernel(
        functools.partial(hold_kernel, cols=cols),
        [
            (conv_weights.shape, low),
            ((2, 3, channels, 3 * channels), low),
            (qkv_weight.shape, low),
            (proj_weight.shape, low),
            ((24, channels), wide),
            ((2, pixels, LANES), wide),
            ((8, pixels), wide),
            ((pixels, LANES), jnp.int32),
            ((8, pixels), jnp.int32),
        ],
        [
            pltpu.SMEM(tile_ids.shape, jnp.int32),
            pltpu.VMEM(norm_gains.shape, wide),
            pltpu.VMEM(norm_shifts.shape, wide),
            pltpu.VMEM(conv_biases.shape, wide),
            pltpu.VMEM(qv_bias.shape, wide),
            pltpu.VMEM((1, channels), wide),
            sem((27,)),
        ],
        [
            tile_ids,
            norm_gains,
            norm_shifts,
            conv_biases,
            conv_weights,
            qkv_weight,
            proj_weight,
            qv_bias,
            proj_bias.reshape(1, channels),
        ],
        "h" * 9,
        conv_flops,
        8,
    )
    held_features[1:] = [
        lax.optimization_barrier((params, block))[1] for block in held_features[1:]
    ]
    pieces = with_cores(held_features)
    far_grad, *pieces[4::2] = lax.optimization_barrier((own_grad, *held_features[2:]))
    held_grads = [own_grad, send_height(own_grad, 2)]
    held_grads[1], pieces[2] = lax.optimization_barrier((held_grads[1], held_features[1]))
    held_grads += [send_height(far_grad, step) for step in steps[1:]]

    all_features, act_one, middle, act_two, residual, table = call_kernel(
        functools.partial(conv_kernel, cols=cols, count=height_size),
        [plane, plane, plane_wide, plane, plane_wide, ((24, channels), wide)],
        [pltpu.VMEM((own_pixels, channels), low), taps, sem],
        [*pieces, held_conv, params, mask],
        "h" + "v" * (height_size + 2),
        2 * conv_flops,
        16,
    )
    residual, *held_grads = lax.optimization_barrier((residual, *held_grads))
    grad_pieces = with_cores(held_grads)
    normed, query, key, value, soft, out_flip, output = call_kernel(
        functools.partial(score_kernel, score_scale=scale),
        [
            plane,
            plane,
            plane,
            plane,
            ((pixels, pixels), low),
            ((channels, pixels), low),
            ((own_pixels, channels), low),
        ],
        [
            flipped,
            *[pltpu.VMEM((pixels, SCORE_ROWS), wide)] * (pixels // SCORE_ROWS),
        ],
        [
            held_qkv,
            held_proj,
            residual,
            table,
            id_rows,
            id_cols,
        ],
        "vvvvvv",
        3 * dot_flops + 2 * score_flops,
        20,
        "v" * 6 + "o",
    )
    normed, *grad_pieces = lax.optimization_barrier((normed, *grad_pieces))
    all_grad, packed, sums, *mixed = call_kernel(
        functools.partial(attention_kernel, score_scale=scale, count=height_size),
        [plane, ((pixels, 3 * channels), low), sums_shape, *mixed_shapes],
        [
            pltpu.VMEM((quarter, 4 * channels), low),
            flipped,
            pltpu.VMEM((pixels, channels), low),
            pltpu.VMEM((pixels, pixels), low),
            pltpu.VMEM((quarter, pixels), low),
            sem((height_size,)),
            *[pltpu.VMEM((pixels, SCORE_ROWS), wide)] * (pixels // SCORE_ROWS),
        ],
        [held_proj, normed, query, key, value, soft, out_flip, *grad_pieces],
        "vvvvvvvh" + "a" * (height_size - 1),
        3 * dot_flops + 4 * score_flops,
        20,
    )
    mixed = trade_canvas(mixed)
    halves = [((18 * out_share, ci_share), low)] * 2
    residual_grad, grad_two, sums, keep_two, send_two = call_kernel(
        functools.partial(third_kernel, cols=cols),
        [plane_wide, plane, sums_shape, *halves],
        [held_wide, narrow, columns, part_held, pltpu.VMEM((8, channels), wide)],
        [held_qkv, all_grad, packed, residual, table, act_two, lane_mask, sums],
        "vvvvvvvv",
        3 * dot_flops + conv_flops // height_size,
        16,
    )
    grad_two, *mixed = lax.optimization_barrier((grad_two, *mixed))
    mixed_sum = mixed[0].astype(wide)
    for piece in mixed[1:]:
        mixed_sum = mixed_sum + piece.astype(wide)
    joints = trade_canvas([mixed_sum.astype(low)] * canvas_size)
    act_two_grad, partial_sums = call_kernel(
        functools.partial(turn_kernel, cols=cols),
        [plane_wide, sums_shape],
        [taps],
        [grad_two, mask, turned, middle, table],
        "vvvvv",
        conv_flops,
        16,
    )
    act_two_grad, *joints = lax.optimization_barrier((act_two_grad, *joints))
    (own_mixed,) = call_kernel(
        place_kernel,
        [((quarter, 4 * channels), low)],
        [],
        joints,
        "v" * canvas_size,
        1,
        12,
    )
    own_mixed, send_two = lax.optimization_barrier((own_mixed, send_two))
    got_two = send_canvas(send_two, 2)
    chip_mixed = send_height(own_mixed, 2)
    core_mixed = send_height(own_mixed, 1)
    grad_one, sums, keep_one, send_one = call_kernel(
        functools.partial(second_kernel, cols=cols),
        [plane, sums_shape, *halves],
        [narrow, columns, part_held, pltpu.VMEM((8, channels), wide)],
        [act_two_grad, partial_sums, middle, table, act_one, lane_mask, sums],
        "vvvvvvv",
        1,
        16,
    )
    got_one = send_canvas(send_one, 1)

    own_total, sums, partial_sums = call_kernel(
        functools.partial(first_kernel, cols=cols),
        [((own_pixels, channels), wide), sums_shape, sums_shape],
        [held_wide, taps],
        [grad_one, all_features, table, mask, sums, turned],
        "vvvvvv",
        1,
        20,
    )
    share_rows = 9 * out_share
    send_rows = share_rows + 2 * sums_shape[0][0] * channels // LANES
    near_sums, far_sums = send_canvas(sums, 1), send_canvas(sums, 3)
    sums, core_mixed, got_one, got_two, far_sums = lax.optimization_barrier(
        (sums, core_mixed, got_one, got_two, far_sums)
    )
    hold_one, send_one, hold_two, send_two = call_kernel(
        halve_sums_kernel,
        [
            ((share_rows, ci_share), wide),
            ((send_rows, ci_share), low),
            ((share_rows, ci_share), wide),
            ((share_rows, ci_share), low),
        ],
        [],
        [keep_one, got_one, keep_two, got_two, sums],
        "vvvvv",
        1,
        12,
    )
    got_two = send_canvas(send_two, 1)
    got_one = send_canvas(send_one, 2)
    chip_mixed, hold_one = lax.optimization_barrier((chip_mixed, hold_one))
    both_mixed = send_height(chip_mixed, 1)
    own_total, hold_one = lax.optimization_barrier((own_total, hold_one))
    (input_grad,) = call_kernel(
        own_kernel,
        [((own_pixels, channels), low)],
        [],
        [own_total, partial_sums, all_features, residual_grad, table],
        "vvvvv",
        dot_flops // 4,
        12,
        "o",
    )
    input_grad, both_mixed = lax.optimization_barrier((input_grad, both_mixed))
    qkv_grad, proj_grad = call_kernel(
        join_kernel,
        [(qkv_weight.shape, wide), (proj_weight.shape, wide)],
        [
            pltpu.VMEM((4, quarter, 3 * channels), wide),
            pltpu.VMEM((4, quarter, channels), wide),
            sem((4, 2)),
        ],
        [own_mixed, chip_mixed, core_mixed, both_mixed],
        "vvvv",
        1,
        12,
        "hh",
    )
    qkv_grad, got_one, got_two, near_sums = lax.optimization_barrier(
        (qkv_grad, got_one, got_two, near_sums)
    )
    vector_shapes = [norm_gains.shape, norm_shifts.shape, conv_biases.shape, qv_bias.shape]
    conv_grad, gains_grad, shifts_grad, biases_grad, qv_grad, proj_bias_grad = call_kernel(
        sums_kernel,
        [((2, 3, 3, out_share, ci_share), wide)]
        + [(shape, wide) for shape in vector_shapes + [(1, channels)]],
        [],
        [sums, near_sums, far_sums, hold_one, got_one, hold_two, got_two],
        "vvvvvvv",
        1,
        12,
        "o" * 6,
    )
    own_shape = (1, local_rows, cols, channels)
    return (
        output.reshape(own_shape),
        input_grad.reshape(own_shape),
        gains_grad,
        shifts_grad,
        jnp.swapaxes(conv_grad, 3, 4),
        biases_grad,
        qkv_grad,
        qv_grad,
        proj_grad,
        proj_bias_grad.reshape(channels),
    )


def on_device(*arrays):
    features, tile_ids = arrays[0], arrays[1]
    local_rows, cols, channels = features.shape[1:]
    pixels = tile_ids.shape[1] * cols
    height_size, canvas_size = lax.axis_size("height"), lax.axis_size("canvas")
    powers = all(size & (size - 1) == 0 for size in (height_size, canvas_size, cols))
    fits = (
        powers
        and height_size > 2
        and canvas_size == 4
        and channels == LANES * canvas_size
        and pixels <= MOST_PIXELS
        and pixels % FILL_ROWS == 0
        and FILL_ROWS % CHUNK == 0
        and pixels % SCORE_ROWS == 0
        and pixels % KEY_ROWS == 0
        and (local_rows * cols) % LANES == 0
        and CHUNK % cols == 0
        and cols % 16 == 0
        and channels % (LANES * canvas_size) == 0
        and 2 * channels == NARROW * height_size
    )
    return whole_canvas(*arrays) if fits else split_canvas(*arrays)


def solution(mesh):
    in_specs = (
        P("canvas", "height", None, None),
        P("canvas", None),
        P(),
        P(),
        P(),
        P(),
        P(),
        P(),
        P(),
        P(),
        P("canvas", "height", None, None),
    )
    out_specs = (
        P("canvas", "height", None, None),
        P("canvas", "height", None, None),
        P(),
        P(),
        P(None, None, None, "canvas", "height"),
        P(),
        P(),
        P(),
        P(),
        P(),
    )
    return jax.shard_map(
        on_device, mesh=mesh, in_specs=in_specs, out_specs=out_specs, check_vma=False
    )
```

```python
import functools

import jax
import jax.numpy as jnp
from jax import lax
from jax.experimental import pallas as pl
from jax.experimental.pallas import tpu as pltpu
from jax.sharding import PartitionSpec as P

GROUPS = 32


epsilon = 1e-06
masked_score = -1e30
MOST_PIXELS = 1024
LANES = 128
NARROW = 128
CHUNK = 128
FILL_ROWS = 256
QUERY_ROWS = 512
SCORE_ROWS = 256
KEY_ROWS = 256


def extended(block, sides, width):
    for axis, dim in sides:
        count = lax.axis_size(axis)
        forward = [(i, i + 1) for i in range(count - 1)]
        backward = [(target, source) for source, target in forward]
        low = lax.ppermute(
            lax.slice_in_dim(block, block.shape[dim] - width, None, axis=dim), axis, forward
        )
        high = lax.ppermute(lax.slice_in_dim(block, 0, width, axis=dim), axis, backward)
        block = jnp.concatenate([low, block, high], axis=dim)
    return block


def group_total(vector):
    return vector.reshape(GROUPS, -1).sum(axis=1)


def spread_groups(vector, channels):
    return jnp.repeat(vector, channels // GROUPS)


def norm_forward(values, gain, shift, members):
    channels = values.shape[1]
    totals = lax.psum(group_total(jnp.sum(values, axis=0)), "height")
    centered = values - spread_groups(totals / members, channels)
    squares = lax.psum(group_total(jnp.sum(centered * centered, axis=0)), "height")
    inverse = spread_groups(lax.rsqrt(squares / members + epsilon), channels)
    normed = centered * inverse
    return (normed, inverse, normed * gain + shift)


def norm_backward(grad_in, normed, inverse, gain, members):
    channels = grad_in.shape[1]
    scaled = grad_in * gain
    both_sums = lax.psum(
        (group_total(jnp.sum(scaled, axis=0)), group_total(jnp.sum(scaled * normed, axis=0))),
        "height",
    )
    mean_grad = spread_groups(both_sums[0] / members, channels)
    mean_cross = spread_groups(both_sums[1] / members, channels)
    result = inverse * (scaled - mean_grad - normed * mean_cross)
    return (result, jnp.sum(grad_in * normed, axis=0), jnp.sum(grad_in, axis=0))


def swish(values):
    return values * jax.nn.sigmoid(values)


def swish_slope(values):
    sigmoid_part = jax.nn.sigmoid(values)
    return sigmoid_part * (1.0 + values * (1.0 - sigmoid_part))


def tap_columns(padded, row_mask, local_rows, canvas_cols):
    pieces = []
    for row_tap in range(3):
        rows_taken = padded[row_tap : row_tap + local_rows] * row_mask[:, row_tap, None, None]
        for col_tap in range(3):
            pieces.append(rows_taken[:, col_tap : col_tap + canvas_cols])
    stacked = jnp.concatenate(pieces, axis=2)
    return stacked.reshape(local_rows * canvas_cols, stacked.shape[2])


def conv_forward(acts, row_mask, weight, bias):
    local_rows, canvas_cols, channels = acts.shape
    rimmed = extended(acts, (("height", 0),), 1)
    padded = jnp.pad(rimmed, ((0, 0), (1, 1), (0, 0)))
    gathered = tap_columns(padded, row_mask, local_rows, canvas_cols)
    result = (
        jnp.dot(
            gathered, weight.reshape(9 * channels, channels), preferred_element_type=jnp.float32
        )
        + bias
    )
    return (result, gathered)


def conv_backward(grad_low, row_mask, weight, gathered):
    local_rows, canvas_cols, channels = grad_low.shape
    flat_grad = grad_low.reshape(local_rows * canvas_cols, channels)
    weight_grad = lax.dot_general(
        gathered, flat_grad, (((0,), (0,)), ((), ())), preferred_element_type=jnp.float32
    )
    rimmed = extended(grad_low, (("height", 0),), 1)
    padded = jnp.pad(rimmed, ((0, 0), (1, 1), (0, 0)))
    grad_taps = tap_columns(padded, row_mask, local_rows, canvas_cols)
    flipped = jnp.transpose(weight[::-1, ::-1], (0, 1, 3, 2)).reshape(9 * channels, channels)
    input_part = jnp.dot(grad_taps, flipped, preferred_element_type=jnp.float32)
    return (
        input_part,
        weight_grad.reshape(3, 3, channels, channels),
        jnp.sum(flat_grad.astype(jnp.float32), axis=0),
    )


def take_rows(array, offset, count):
    return lax.dynamic_slice_in_dim(array, offset, count)


def score_grads(
    queries, out_grad, log_total, row_dots, query_ids, key_rows, value_rows, key_ids, score_scale
):
    scores = (
        lax.dot_general(
            queries, key_rows, (((1,), (1,)), ((), ())), preferred_element_type=jnp.float32
        )
        * score_scale
    )
    same_tile = query_ids[:, None] == key_ids[None, :]
    softmax_block = jnp.exp(jnp.where(same_tile, scores - log_total[:, None], masked_score))
    weight_grad = lax.dot_general(
        out_grad, value_rows, (((1,), (1,)), ((), ())), preferred_element_type=jnp.float32
    )
    score_grad = (softmax_block * (weight_grad - row_dots[:, None])).astype(jnp.bfloat16)
    return (softmax_block.astype(jnp.bfloat16), score_grad)


def split_canvas(
    features,
    tile_ids,
    norm_gains,
    norm_shifts,
    conv_weights,
    conv_biases,
    qkv_weight,
    qv_bias,
    proj_weight,
    proj_bias,
    cotangent,
):
    height_size = lax.axis_size("height")
    local_rows = features.shape[1]
    canvas_cols = features.shape[2]
    channels = features.shape[3]
    pixels = local_rows * canvas_cols
    row_ids = tile_ids[0]
    all_rows = row_ids.shape[0]
    members = float(all_rows * canvas_cols * (channels // GROUPS))
    score_scale = channels ** (-0.5)
    first_row = lax.axis_index("height") * local_rows
    edge_ids = jnp.full((1,), -1, jnp.int32)
    padded_ids = jnp.concatenate([edge_ids, row_ids, edge_ids])
    near_ids = lax.dynamic_slice_in_dim(padded_ids, first_row, local_rows + 2)
    own_rows = near_ids[1 : local_rows + 1]
    row_mask = jnp.stack(
        [near_ids[row_tap : row_tap + local_rows] == own_rows for row_tap in range(3)], axis=1
    ).astype(jnp.bfloat16)
    key_ids = jnp.repeat(row_ids, canvas_cols)
    query_ids = jnp.repeat(own_rows, canvas_cols)
    grid_shape = (local_rows, canvas_cols, channels)
    inputs = features[0].reshape(pixels, channels).astype(jnp.float32)
    normed_one, inverse_one, pre_one = norm_forward(inputs, norm_gains[0], norm_shifts[0], members)
    act_one = swish(pre_one).astype(jnp.bfloat16).reshape(grid_shape)
    middle, taps_one = conv_forward(act_one, row_mask, conv_weights[0], conv_biases[0])
    normed_two, inverse_two, pre_two = norm_forward(middle, norm_gains[1], norm_shifts[1], members)
    act_two = swish(pre_two).astype(jnp.bfloat16).reshape(grid_shape)
    branch, taps_two = conv_forward(act_two, row_mask, conv_weights[1], conv_biases[1])
    residual = inputs + branch
    normed_three, inverse_three, pre_three = norm_forward(
        residual, norm_gains[2], norm_shifts[2], members
    )
    attn_input = pre_three.astype(jnp.bfloat16)
    mixed = jnp.dot(attn_input, qkv_weight, preferred_element_type=jnp.float32)
    queries = (mixed[:, :channels] + qv_bias[0]).astype(jnp.bfloat16)
    key_rows = mixed[:, channels : 2 * channels].astype(jnp.bfloat16)
    value_rows = (mixed[:, 2 * channels :] + qv_bias[1]).astype(jnp.bfloat16)
    running_max = jnp.full((pixels,), masked_score, jnp.float32)
    key_piece = lax.all_gather(key_rows, "height", axis=0, tiled=True)
    value_piece = lax.all_gather(value_rows, "height", axis=0, tiled=True)
    scores = (
        lax.dot_general(
            queries, key_piece, (((1,), (1,)), ((), ())), preferred_element_type=jnp.float32
        )
        * score_scale
    )
    same_tile = query_ids[:, None] == key_ids[None, :]
    scores = jnp.where(same_tile, scores, masked_score)
    new_max = jnp.maximum(running_max, jnp.max(scores, axis=1))
    weights = jnp.where(same_tile, jnp.exp(scores - new_max[:, None]), 0.0)
    summed_out = jnp.dot(
        weights.astype(jnp.bfloat16), value_piece, preferred_element_type=jnp.float32
    )
    total_weight = jnp.sum(weights, axis=1)
    log_total = new_max + jnp.log(total_weight)
    attended = summed_out / total_weight[:, None]
    attended_low = attended.astype(jnp.bfloat16)
    output = (
        residual
        + jnp.dot(attended_low, proj_weight, preferred_element_type=jnp.float32)
        + proj_bias
    )
    out_grad = cotangent[0].reshape(pixels, channels)
    out_grad_full = out_grad.astype(jnp.float32)
    proj_grad = lax.dot_general(
        attended_low, out_grad, (((0,), (0,)), ((), ())), preferred_element_type=jnp.float32
    )
    proj_bias_grad = jnp.sum(out_grad_full, axis=0)
    attended_grad = lax.dot_general(
        out_grad, proj_weight, (((1,), (1,)), ((), ())), preferred_element_type=jnp.float32
    ).astype(jnp.bfloat16)
    row_dots = jnp.sum(attended_grad.astype(jnp.float32) * attended, axis=1)
    block_rows = pixels * min(height_size, 8)
    zero_block = jnp.zeros((pixels, channels), jnp.float32)
    key_all, value_all = (
        lax.all_gather(key_rows, "height", axis=0, tiled=True),
        lax.all_gather(value_rows, "height", axis=0, tiled=True),
    )
    query_all, grad_all = (
        lax.all_gather(queries, "height", axis=0, tiled=True),
        lax.all_gather(attended_grad, "height", axis=0, tiled=True),
    )
    total_all, dots_all = (
        lax.all_gather(log_total, "height", axis=0, tiled=True),
        lax.all_gather(row_dots, "height", axis=0, tiled=True),
    )

    def own_query_step(running, block_index):
        offset = block_index * block_rows
        key_part = take_rows(key_all, offset, block_rows)
        rounded, score_grad = score_grads(
            queries,
            attended_grad,
            log_total,
            row_dots,
            query_ids,
            key_part,
            take_rows(value_all, offset, block_rows),
            take_rows(key_ids, offset, block_rows),
            score_scale,
        )
        return (
            running
            + jnp.dot(score_grad, key_part, preferred_element_type=jnp.float32) * score_scale,
            None,
        )

    def own_key_step(running, block_index):
        offset = block_index * block_rows
        query_part = take_rows(query_all, offset, block_rows)
        grad_part = take_rows(grad_all, offset, block_rows)
        rounded, score_grad = score_grads(
            query_part,
            grad_part,
            take_rows(total_all, offset, block_rows),
            take_rows(dots_all, offset, block_rows),
            take_rows(key_ids, offset, block_rows),
            key_rows,
            value_rows,
            query_ids,
            score_scale,
        )
        key_part = (
            lax.dot_general(
                score_grad, query_part, (((0,), (0,)), ((), ())), preferred_element_type=jnp.float32
            )
            * score_scale
        )
        value_part = lax.dot_general(
            rounded, grad_part, (((0,), (0,)), ((), ())), preferred_element_type=jnp.float32
        )
        return ((running[0] + key_part, running[1] + value_part), None)

    block_count = key_all.shape[0] // block_rows
    query_grad, unused_one = lax.scan(own_query_step, zero_block, jnp.arange(block_count))
    (key_grad, value_grad), unused_two = lax.scan(
        own_key_step, (zero_block, zero_block), jnp.arange(block_count)
    )
    query_low = query_grad.astype(jnp.bfloat16)
    key_low = key_grad.astype(jnp.bfloat16)
    value_low = value_grad.astype(jnp.bfloat16)
    stacked_grad = jnp.concatenate([query_low, key_low, value_low], axis=1)
    qkv_grad = lax.dot_general(
        attn_input, stacked_grad, (((0,), (0,)), ((), ())), preferred_element_type=jnp.float32
    )
    qv_grad = jnp.stack(
        [
            jnp.sum(query_low.astype(jnp.float32), axis=0),
            jnp.sum(value_low.astype(jnp.float32), axis=0),
        ]
    )
    normed_grad = lax.dot_general(
        stacked_grad, qkv_weight, (((1,), (1,)), ((), ())), preferred_element_type=jnp.float32
    )
    back_three, gain_three, shift_three = norm_backward(
        normed_grad, normed_three, inverse_three, norm_gains[2], members
    )
    residual_grad = out_grad_full + back_three
    grad_two = residual_grad.astype(jnp.bfloat16).reshape(grid_shape)
    act_two_grad, weight_two_grad, bias_two_grad = conv_backward(
        grad_two, row_mask, conv_weights[1], taps_two
    )
    middle_grad, gain_two, shift_two = norm_backward(
        act_two_grad * swish_slope(pre_two), normed_two, inverse_two, norm_gains[1], members
    )
    grad_one = middle_grad.astype(jnp.bfloat16).reshape(grid_shape)
    act_one_grad, weight_one_grad, bias_one_grad = conv_backward(
        grad_one, row_mask, conv_weights[0], taps_one
    )
    input_back, gain_one, shift_one = norm_backward(
        act_one_grad * swish_slope(pre_one), normed_one, inverse_one, norm_gains[0], members
    )
    input_grad = residual_grad + input_back
    conv_grad = jnp.stack([weight_one_grad, weight_two_grad])
    conv_part = lax.psum_scatter(conv_grad, "height", scatter_dimension=4, tiled=True)
    conv_part = lax.psum_scatter(
        conv_part.astype(jnp.bfloat16), "canvas", scatter_dimension=3, tiled=True
    ).astype(jnp.float32)
    summed = lax.psum(
        (
            jnp.stack([gain_one, gain_two, gain_three]),
            jnp.stack([shift_one, shift_two, shift_three]),
            jnp.stack([bias_one_grad, bias_two_grad]),
            qkv_grad,
            qv_grad,
            proj_grad,
            proj_bias_grad,
        ),
        ("canvas", "height"),
    )
    return (
        output.astype(jnp.bfloat16).reshape((1,) + grid_shape),
        input_grad.astype(jnp.bfloat16).reshape((1,) + grid_shape),
        summed[0],
        summed[1],
        conv_part,
        summed[2],
        summed[3],
        summed[4],
        summed[5],
        summed[6],
    )


def fold(block):
    rows, width = block.shape
    return jnp.sum(block.reshape(rows // 8, 8, width), axis=0)


def group_lanes(block, group):
    lane = lax.broadcasted_iota(jnp.int32, block.shape, 1)
    width = block.shape[1]
    step = 1
    while step < group:
        above = pltpu.roll(block, step, 1)
        below = pltpu.roll(block, width - step, 1)
        block = block + jnp.where((lane & step) != 0, above, below)
        step *= 2
    return block


def group_mean(partial, members):
    spread = group_lanes(partial, partial.shape[1] // GROUPS)
    return jnp.sum(spread, axis=0, keepdims=True) * (1.0 / members)


def widen(block, width):
    return jnp.concatenate([block] * (width // block.shape[1]), axis=1)


def each_block(pixels, block, body, carry=0):
    def step(index, carry):
        return body(pl.ds(pl.multiple_of(index * block, block), block), carry)

    return lax.fori_loop(0, pixels // block, step, carry)


def each_chunk(pixels, body, carry):
    return each_block(pixels, CHUNK, body, carry)


def aligned(start, step):
    return start if isinstance(start, int) else pl.multiple_of(start, step)


class RunningStats:
    def __init__(self, channels):
        self.width = channels // GROUPS
        self.reference = None
        self.sums = self.squares = jnp.zeros((8, channels), jnp.float32)

    def add(self, block):
        if self.reference is None:
            self.reference = group_mean(block[0:8], 8.0 * self.width)
        offset = block - self.reference
        self.sums = self.sums + fold(offset)
        self.squares = self.squares + fold(offset * offset)

    def finish(self, pixels):
        both = group_lanes(jnp.concatenate([self.sums, self.squares], axis=0), self.width)
        share = 1.0 / (pixels * self.width)
        offset = column_total(both[0:8]) * share
        variance = column_total(both[8:16]) * share - offset * offset
        return self.reference + offset, lax.rsqrt(jnp.maximum(variance, 0.0) + epsilon)


def put_taps(taps_ref, block, rows, cols):
    count, channels = block.shape
    place = lax.broadcasted_iota(jnp.int32, block.shape, 0) & (cols - 1)
    left = jnp.where(place == 0, 0.0, pltpu.roll(block, 1, 0))
    right = jnp.where(place == cols - 1, 0.0, pltpu.roll(block, count - 1, 0))
    inner = pl.ds(aligned(rows.start + cols, cols), count)
    taps_ref[inner, 0:channels] = left.astype(jnp.bfloat16)
    taps_ref[inner, channels : 2 * channels] = block.astype(jnp.bfloat16)
    taps_ref[inner, 2 * channels :] = right.astype(jnp.bfloat16)


def clear_edges(taps_ref, cols):
    edge = jnp.zeros((cols, taps_ref.shape[1]), taps_ref.dtype)
    taps_ref[0:cols, :] = edge
    taps_ref[taps_ref.shape[0] - cols :, :] = edge


def begin_conv(taps_ref, product, total_ref, fill, first, cols):
    for start in range(0, total_ref.shape[0], FILL_ROWS):
        for inner in range(start, start + FILL_ROWS, CHUNK):
            fill(pl.ds(inner, CHUNK))
        rows = pl.ds(start, FILL_ROWS)
        total_ref[rows, :] = first(rows, product(taps_ref, pl.ds(start + cols, FILL_ROWS), 1))


def add_rows(taps_ref, product, mask_ref, total_ref, row_tap, last, cols, old_ref=None):
    pixels, channels = total_ref.shape
    old_ref = total_ref if old_ref is None else old_ref
    for start in range(0, pixels, FILL_ROWS):
        rows = slice(start, start + FILL_ROWS)
        part = product(taps_ref, pl.ds(start + row_tap * cols, FILL_ROWS), row_tap)
        mask = widen(mask_ref[row_tap // 2, rows, :], channels)
        total_ref[rows, :] = last(rows, old_ref[rows, :] + mask * part)


def run_conv(taps_ref, product, mask_ref, total_ref, fill, first, last, cols):
    begin_conv(taps_ref, product, total_ref, fill, first, cols)
    add_rows(taps_ref, product, mask_ref, total_ref, 0, lambda rows, value: value, cols)
    add_rows(taps_ref, product, mask_ref, total_ref, 2, last, cols)


def product_forward(weight_ref):
    channels = weight_ref.shape[-1]

    def product(taps_ref, shifted, row_tap):
        return jnp.dot(
            taps_ref[shifted, :],
            weight_ref[row_tap].reshape(3 * channels, channels),
            preferred_element_type=jnp.float32,
        )

    return product


def product_backward(weight_ref):
    def product(taps_ref, shifted, row_tap):
        return lax.dot_general(
            taps_ref[shifted, :],
            weight_ref[row_tap],
            (((1,), (1,)), ((), ())),
            preferred_element_type=jnp.float32,
        )

    return product


def activation(read, mean, inverse, gain, shift, act_ref, taps_ref, cols):
    scale, offset = 0.5 * inverse * gain, 0.5 * shift

    def fill(rows):
        half = (read(rows) - mean) * scale + offset
        act = half * (1.0 + jnp.tanh(half))
        act_ref[rows, :] = act.astype(jnp.bfloat16)
        put_taps(taps_ref, act, rows, cols)

    return fill


def back_means(sums, gain, pixels):
    channels = gain.shape[1]
    members = float(pixels * (channels // GROUPS))
    return group_mean(sums[0] * gain, members), group_mean(sums[1] * gain, members)


def column_total(partial):
    return jnp.sum(partial, axis=0, keepdims=True)


def weight_part(act_ref, narrow, lanes_ref, flip_ref, columns_ref, part_ref, cols):
    pixels, channels = act_ref.shape
    height = lax.axis_index("height")
    share = NARROW // 2
    flip_ref[...] = narrow.T
    own = pl.ds(pl.multiple_of((height % 2) * share, share), share)
    grad = flip_ref[own, :].astype(jnp.float32)
    column = lax.broadcasted_iota(jnp.int32, grad.shape, 1) & (cols - 1)
    for col_tap in range(3):
        shifted = grad
        if col_tap == 0:
            shifted = jnp.where(column == cols - 1, 0.0, pltpu.roll(grad, pixels - 1, 1))
        elif col_tap == 2:
            shifted = jnp.where(column == 0, 0.0, pltpu.roll(grad, 1, 1))
        for row_tap in range(3):
            tap = 3 * row_tap + col_tap
            place = slice(tap * share, (tap + 1) * share)
            if row_tap == 1:
                columns_ref[place, :] = shifted.astype(jnp.bfloat16)
                continue
            side, turn = (0, pixels - cols) if row_tap == 0 else (1, cols)
            masked = (shifted * lanes_ref[side : side + 1, :]).astype(jnp.bfloat16)
            columns_ref[place, :] = pltpu.roll(masked, turn, 1)
    part_ref[...] = jnp.dot(
        columns_ref[...], act_ref[...], preferred_element_type=jnp.float32
    ).astype(jnp.bfloat16)


def begin_back(grad_ref, weights_ref, mask_ref, taps_ref, total_ref, cols):
    clear_edges(taps_ref, cols)

    def fill(rows):
        put_taps(taps_ref, grad_ref[rows, :].astype(jnp.float32), rows, cols)

    product = product_backward(weights_ref)
    begin_conv(taps_ref, product, total_ref, fill, lambda rows, part: part, cols)
    add_rows(taps_ref, product, mask_ref, total_ref, 0, lambda rows, value: value, cols)


def finish_back(
    weights_ref, mask_ref, taps_ref, total_ref, read, table_ref, which, cols, old_ref=None
):
    mean, inverse, gain, shift = norm_rows(table_ref, which)
    scale, offset = 0.5 * inverse * gain, 0.5 * shift
    sums = []

    def slope(rows, value):
        centered = read(rows) - mean
        half = centered * scale + offset
        turn = jnp.tanh(half)
        double = value * ((1.0 + turn) * (1.0 + half * (1.0 - turn)))
        sums.append((fold(double), fold(double * centered)))
        return double

    add_rows(
        taps_ref, product_backward(weights_ref), mask_ref, total_ref, 2, slope, cols, old_ref
    )
    plain, cross = sum(pair[0] for pair in sums), sum(pair[1] for pair in sums)
    return 0.5 * plain, 0.5 * inverse * cross


def norm_back(total_ref, double, sums, read, table_ref, which, pixels, scales_ref=None):
    mean, inverse, gain, shift = norm_rows(table_ref, which)
    mean_grad, mean_cross = back_means(sums, gain, pixels)
    slope = inverse * gain * (0.5 if double else 1.0)
    level, tilt = inverse * mean_grad, inverse * inverse * mean_cross
    if scales_ref is not None:
        for row, scales in enumerate((mean, slope, level, tilt)):
            scales_ref[row : row + 1, :] = scales

    def back(rows, inner):
        return total_ref[inner, :] * slope - level - (read(rows) - mean) * tilt

    return back


def own_lanes():
    block = lax.axis_index("height") // 2
    return pl.ds(pl.multiple_of(block * NARROW, NARROW), NARROW)


def narrow_back(total_ref, value_ref, scales_ref):
    lanes = own_lanes()
    mean, slope, level, tilt = (scales_ref[row : row + 1, lanes] for row in range(4))
    return total_ref[:, lanes] * slope - level - (value_ref[:, lanes] - mean) * tilt


def turn_kernel(grad_ref, mask_ref, weights_ref, total_ref, taps_ref, *, cols):
    begin_back(grad_ref, weights_ref.at[1], mask_ref, taps_ref, total_ref, cols)


def norm_rows(table_ref, which):
    picks = (2 * which, 2 * which + 1, 6 + which, 9 + which)
    return tuple(table_ref[pick : pick + 1, :] for pick in picks)


def build_masks(ids_ref, mask_ref, lanes_ref, id_rows_ref, id_cols_ref, cols):
    rows = ids_ref.shape[1]
    for row in range(rows):
        here = ids_ref[0, row]
        place = slice(row * cols, (row + 1) * cols)
        id_rows_ref[place, :] = jnp.full((cols, LANES), here, jnp.int32)
        for side, other in ((0, row - 1), (1, row + 1)):
            same = jnp.float32(0.0)
            if 0 <= other < rows:
                same = jnp.where(ids_ref[0, other] == here, 1.0, 0.0).astype(jnp.float32)
            mask_ref[side, place, :] = jnp.full((cols, LANES), same, jnp.float32)
    lane = lax.broadcasted_iota(jnp.int32, (8, LANES), 1)
    each = LANES // cols
    for block in range(rows // each):
        ids = jnp.full((8, LANES), ids_ref[0, block * each], jnp.int32)
        for step in range(1, each):
            ids = jnp.where(lane >= step * cols, ids_ref[0, block * each + step], ids)
        id_cols_ref[:, block * LANES : (block + 1) * LANES] = ids
    ids = id_cols_ref[...].astype(jnp.float32)
    pixels = ids.shape[1]
    pixel = lax.broadcasted_iota(jnp.int32, ids.shape, 1)
    above = jnp.where(pixel < cols, -1.0, pltpu.roll(ids, cols, 1))
    below = jnp.where(pixel >= pixels - cols, -1.0, pltpu.roll(ids, pixels - cols, 1))
    lanes_ref[0:1, :] = jnp.where(above == ids, 1.0, 0.0)[0:1]
    lanes_ref[1:2, :] = jnp.where(below == ids, 1.0, 0.0)[0:1]


def place_pieces(pieces, whole_ref, sems):
    own_pixels = whole_ref.shape[0] // len(pieces)
    height = lax.axis_index("height")
    copies = []
    for place, piece in enumerate(pieces):
        start = pl.multiple_of((height ^ place) * own_pixels, own_pixels)
        rows = pl.ds(start, own_pixels)
        copies.append(pltpu.make_async_copy(piece, whole_ref.at[rows, :], sems.at[place]))
    return copies


def hold_kernel(
    ids_hbm,
    gains_hbm,
    shifts_hbm,
    biases_hbm,
    weights_hbm,
    qkv_hbm,
    proj_hbm,
    qv_bias_hbm,
    proj_bias_hbm,
    weights_ref,
    turned_ref,
    qkv_ref,
    proj_ref,
    table_ref,
    mask_ref,
    lanes_ref,
    id_rows_ref,
    id_cols_ref,
    ids_ref,
    gains_ref,
    shifts_ref,
    biases_ref,
    qv_bias_ref,
    proj_bias_ref,
    sems,
    *,
    cols,
):
    channels = weights_ref.shape[-1]
    small = [
        (ids_hbm, ids_ref),
        (gains_hbm, gains_ref),
        (shifts_hbm, shifts_ref),
        (biases_hbm, biases_ref),
        (qv_bias_hbm, qv_bias_ref),
        (proj_bias_hbm, proj_bias_ref),
    ]
    large = [(weights_hbm, weights_ref), (qkv_hbm, qkv_ref), (proj_hbm, proj_ref)]
    for which in range(2):
        for row_tap in range(3):
            for col_tap in range(3):
                place = slice(col_tap * channels, (col_tap + 1) * channels)
                large.append(
                    (
                        weights_hbm.at[which, 2 - row_tap, 2 - col_tap],
                        turned_ref.at[which, row_tap, :, place],
                    )
                )
    copies = [
        pltpu.make_async_copy(source, target, sems.at[index])
        for index, (source, target) in enumerate(small + large)
    ]
    for copy in copies:
        copy.start()
    for copy in copies[: len(small)]:
        copy.wait()
    build_masks(ids_ref, mask_ref, lanes_ref, id_rows_ref, id_cols_ref, cols)
    table_ref[6:9, :] = gains_ref[...]
    table_ref[9:12, :] = shifts_ref[...]
    table_ref[12:14, :] = biases_ref[...]
    table_ref[14:16, :] = qv_bias_ref[...]
    table_ref[16:17, :] = proj_bias_ref[...]
    for copy in copies[len(small) :]:
        copy.wait()


def conv_kernel(*refs, cols, count):
    pieces, refs = refs[:count], refs[count:]
    (
        weights_ref,
        params_ref,
        mask_ref,
        features_ref,
        act_one_ref,
        middle_ref,
        act_two_ref,
        residual_ref,
        table_ref,
        own_ref,
        taps_ref,
        sem,
    ) = refs
    pixels, channels = features_ref.shape
    wide = jnp.float32
    own_copy = pltpu.make_async_copy(pieces[0], own_ref, sem)
    own_copy.start()
    table_ref[...] = params_ref[...]
    clear_edges(taps_ref, cols)

    def read_input(rows):
        return features_ref[rows, :].astype(wide)

    def read_middle(rows):
        return middle_ref[rows, :]

    height = lax.axis_index("height")
    own_pixels = pixels // count
    seen = RunningStats(channels)
    for place in list(range(1, count)) + [0]:
        if place == 0:
            own_copy.wait()
        piece = (pieces[place] if place else own_ref)[...]
        start = pl.multiple_of((height ^ place) * own_pixels, own_pixels)
        features_ref[pl.ds(start, own_pixels), :] = piece
        seen.add(piece.astype(wide))
    table_ref[0:1, :], table_ref[1:2, :] = seen.finish(pixels)
    seen = RunningStats(channels)

    def keep(rows, value):
        seen.add(value)
        return value

    run_conv(
        taps_ref,
        product_forward(weights_ref.at[0]),
        mask_ref,
        middle_ref,
        activation(read_input, *norm_rows(table_ref, 0), act_one_ref, taps_ref, cols),
        lambda rows, part: part + table_ref[12:13, :],
        keep,
        cols,
    )
    table_ref[2:3, :], table_ref[3:4, :] = seen.finish(pixels)
    seen = RunningStats(channels)
    run_conv(
        taps_ref,
        product_forward(weights_ref.at[1]),
        mask_ref,
        residual_ref,
        activation(read_middle, *norm_rows(table_ref, 1), act_two_ref, taps_ref, cols),
        lambda rows, part: part + (read_input(rows) + table_ref[13:14, :]),
        keep,
        cols,
    )
    table_ref[4:5, :], table_ref[5:6, :] = seen.finish(pixels)


def score_kernel(
    qkv_ref,
    proj_ref,
    residual_ref,
    table_ref,
    id_rows_ref,
    id_cols_ref,
    normed_ref,
    query_ref,
    key_ref,
    value_ref,
    soft_ref,
    out_flip_ref,
    output_ref,
    value_flip_ref,
    *scores_refs,
    score_scale,
):
    pixels, channels = residual_ref.shape
    own_pixels = output_ref.shape[0]
    wide = jnp.float32
    exponent = score_scale * 1.4426950408889634
    mean, inverse, gain, shift = norm_rows(table_ref, 2)
    scale = inverse * gain

    def project(rows, carry):
        normed = ((residual_ref[rows, :] - mean) * scale + shift).astype(jnp.bfloat16)
        normed_ref[rows, :] = normed
        query_ref[rows, :] = (
            jnp.dot(normed, qkv_ref[:, 0:channels], preferred_element_type=wide)
            + table_ref[14:15, :]
        ).astype(jnp.bfloat16)
        key_ref[rows, :] = jnp.dot(
            normed, qkv_ref[:, channels : 2 * channels], preferred_element_type=wide
        ).astype(jnp.bfloat16)
        values = (
            jnp.dot(normed, qkv_ref[:, 2 * channels :], preferred_element_type=wide)
            + table_ref[15:16, :]
        ).astype(jnp.bfloat16)
        value_ref[rows, :] = values
        value_flip_ref[:, rows] = values.T
        return carry

    each_block(pixels, min(QUERY_ROWS, pixels), project)
    block = scores_refs[0].shape[1]
    steps = range(0, pixels, KEY_ROWS)

    def score(index):
        rows = slice(index * block, (index + 1) * block)
        for start in steps:
            keys = slice(start, start + KEY_ROWS)
            scores = lax.dot_general(
                key_ref[keys, :],
                query_ref[rows, :],
                (((1,), (1,)), ((), ())),
                preferred_element_type=wide,
            )
            same = widen(id_rows_ref[keys, :], block) == id_cols_ref[0:1, rows]
            scores_refs[index][keys, :] = jnp.where(same, scores, masked_score)

    def soften(index):
        rows = slice(index * block, (index + 1) * block)
        scores_ref = scores_refs[index]
        peak = jnp.full((8, block), masked_score, wide)
        for start in steps:
            scores = scores_ref[start : start + KEY_ROWS, :]
            peak = jnp.maximum(peak, jnp.max(scores.reshape(-1, 8, block), axis=0))
        peak = jnp.max(peak, axis=0, keepdims=True)
        total = jnp.zeros((8, block), wide)
        for start in steps:
            keys = slice(start, start + KEY_ROWS)
            powers = jnp.exp2((scores_ref[keys, :] - peak) * exponent)
            scores_ref[keys, :] = powers
            total = total + fold(powers)
        share = 1.0 / column_total(total)
        for start in steps:
            keys = slice(start, start + KEY_ROWS)
            soft_ref[keys, rows] = (scores_ref[keys, :] * share).astype(jnp.bfloat16)

    score(0)
    for index in range(len(scores_refs)):
        if index + 1 < len(scores_refs):
            score(index + 1)
        soften(index)

    def collect(rows, carry):
        out_flip_ref[rows, :] = jnp.dot(
            value_flip_ref[rows, :], soft_ref[...], preferred_element_type=wide
        ).astype(jnp.bfloat16)
        return carry

    each_block(channels, channels // 2, collect)
    height = lax.axis_index("height")
    own = pl.ds(pl.multiple_of(height * own_pixels, own_pixels), own_pixels)
    output_ref[...] = (
        residual_ref[own, :]
        + lax.dot_general(
            out_flip_ref[:, own],
            proj_ref[...],
            (((0,), (0,)), ((), ())),
            preferred_element_type=wide,
        )
        + table_ref[16:17, :]
    ).astype(jnp.bfloat16)


def own_quarter():
    height = lax.axis_index("height")
    return (height & 1) * 2 + ((height >> 1) & 1)


def send_order(source_ref, targets, axis, share):
    me = lax.axis_index("canvas")
    for step, target in enumerate(targets):
        place = pl.ds(pl.multiple_of((me ^ step) * share, share), share)
        target[...] = source_ref[place, :] if axis == 0 else source_ref[:, place]


def attention_kernel(
    proj_ref,
    normed_ref,
    query_ref,
    key_ref,
    value_ref,
    soft_ref,
    out_flip_ref,
    *refs,
    score_scale,
    count,
):
    pieces, (grad_ref, packed_ref, sums_ref), refs = (
        refs[:count],
        refs[count : count + 3],
        refs[count + 3 :],
    )
    pixels, channels = normed_ref.shape
    blocks = pixels // SCORE_ROWS
    grads_refs, refs = refs[-blocks:], refs[:-blocks]
    *mixed_refs, mixed_ref, key_flip_ref, back_ref, score_grad_ref, flip_ref, sems = refs
    wide = jnp.float32
    copies = place_pieces(pieces, grad_ref, sems)
    for copy in copies:
        copy.start()
    quarter = channels // 4
    own = pl.ds(pl.multiple_of(own_quarter() * quarter, quarter), quarter)
    flip_ref[...] = normed_ref[:, own].T
    key_flip_ref[...] = key_ref[...].T
    for copy in copies:
        copy.wait()
    block, count = SCORE_ROWS, blocks
    steps = range(0, pixels, KEY_ROWS)

    def block_rows(index):
        return slice(index * block, (index + 1) * block)

    for index in range(count):
        back_ref[block_rows(index), :] = lax.dot_general(
            grad_ref[block_rows(index), :],
            proj_ref[...],
            (((1,), (1,)), ((), ())),
            preferred_element_type=wide,
        ).astype(jnp.bfloat16)

    def weigh(index):
        total = jnp.zeros((8, block), wide)
        for start in steps:
            keys = slice(start, start + KEY_ROWS)
            weight_grad = lax.dot_general(
                value_ref[keys, :],
                back_ref[block_rows(index), :],
                (((1,), (1,)), ((), ())),
                preferred_element_type=wide,
            )
            grads_refs[index][keys, :] = weight_grad
            total = total + fold(soft_ref[keys, block_rows(index)].astype(wide) * weight_grad)
        return column_total(total)

    def slope(index, dots):
        for start in steps:
            keys = slice(start, start + KEY_ROWS)
            weights = soft_ref[keys, block_rows(index)].astype(wide)
            score_grad_ref[keys, block_rows(index)] = (
                weights * (grads_refs[index][keys, :] - dots)
            ).astype(jnp.bfloat16)

    dots = weigh(0)
    for index in range(count):
        now, rows = dots, block_rows(index)
        if index + 1 < count:
            dots = weigh(index + 1)
        slope(index, now)
        packed_ref[rows, 2 * channels :] = jnp.dot(
            soft_ref[rows, :], back_ref[...], preferred_element_type=wide
        ).astype(jnp.bfloat16)
        query_grad = jnp.dot(
            key_flip_ref[...], score_grad_ref[:, rows], preferred_element_type=wide
        )
        packed_ref[rows, 0:channels] = (query_grad * score_scale).astype(jnp.bfloat16).T
    for index in range(count):
        rows = block_rows(index)
        packed_ref[rows, channels : 2 * channels] = (
            jnp.dot(score_grad_ref[rows, :], query_ref[...], preferred_element_type=wide)
            * score_scale
        ).astype(jnp.bfloat16)

    def pack(rows, carry):
        return (
            carry[0] + fold(packed_ref[rows, 0:channels].astype(wide)),
            carry[1] + fold(packed_ref[rows, 2 * channels :].astype(wide)),
            carry[2] + fold(grad_ref[rows, :].astype(wide)),
        )

    zeros = jnp.zeros((8, channels), wide)
    totals = zeros, zeros, zeros
    for start in range(0, pixels, CHUNK):
        totals = pack(pl.ds(start, CHUNK), totals)
    sums_ref[...] = jnp.zeros(sums_ref.shape, wide)
    for row, total in enumerate(totals):
        sums_ref[8 + row : 9 + row, :] = column_total(total)
    mixed_ref[:, 0 : 3 * channels] = jnp.dot(
        flip_ref[...], packed_ref[...], preferred_element_type=wide
    ).astype(jnp.bfloat16)
    mixed_ref[:, 3 * channels :] = jnp.dot(
        out_flip_ref[own, :], grad_ref[...], preferred_element_type=wide
    ).astype(jnp.bfloat16)
    send_order(mixed_ref, mixed_refs, 0, quarter // len(mixed_refs))


def third_kernel(
    qkv_ref,
    grad_ref,
    packed_ref,
    residual_ref,
    table_ref,
    act_two_ref,
    lanes_ref,
    old_sums_ref,
    residual_grad_ref,
    grad_two_ref,
    sums_ref,
    keep_ref,
    send_ref,
    total_ref,
    flip_ref,
    columns_ref,
    part_ref,
    scales_ref,
    *,
    cols,
):
    pixels, channels = residual_ref.shape
    block = FILL_ROWS
    wide = jnp.float32
    mean, inverse, gain, shift = norm_rows(table_ref, 2)
    zeros = jnp.zeros((8, channels), wide)

    sums = (zeros, zeros)
    for start in range(0, pixels, block):
        rows = pl.ds(start, block)
        normed_grad = lax.dot_general(
            packed_ref[rows, :], qkv_ref[...], (((1,), (1,)), ((), ())), preferred_element_type=wide
        )
        total_ref[rows, :] = normed_grad
        centered = residual_ref[rows, :] - mean
        sums = sums[0] + fold(normed_grad), sums[1] + fold(normed_grad * centered)
    sums = sums[0], sums[1] * inverse
    sums_ref[...] = old_sums_ref[...]
    sums_ref[5:6, :] = column_total(sums[1])
    sums_ref[6:7, :] = column_total(sums[0])
    back = norm_back(
        total_ref, False, sums, lambda rows: residual_ref[rows, :], table_ref, 2, pixels, scales_ref
    )
    narrow = narrow_back(total_ref, residual_ref, scales_ref)
    narrow = (grad_ref[:, own_lanes()].astype(wide) + narrow).astype(jnp.bfloat16)
    weight_part(act_two_ref, narrow, lanes_ref, flip_ref, columns_ref, part_ref, cols)

    def finish(rows, carry):
        total = grad_ref[rows, :].astype(wide) + back(rows, rows)
        residual_grad_ref[rows, :] = total
        low = total.astype(jnp.bfloat16)
        grad_two_ref[rows, :] = low
        return carry + fold(low.astype(wide))

    total = zeros
    for start in range(0, pixels, CHUNK):
        total = finish(pl.ds(start, CHUNK), total)
    sums_ref[7:8, :] = column_total(total)
    keep_half(part_ref, 2, 1, keep_ref, send_ref)


def second_kernel(
    old_total_ref,
    taps_ref,
    middle_ref,
    table_ref,
    act_one_ref,
    mask_ref,
    lanes_ref,
    weights_ref,
    old_sums_ref,
    grad_one_ref,
    sums_ref,
    keep_ref,
    send_ref,
    total_ref,
    flip_ref,
    columns_ref,
    part_ref,
    scales_ref,
    *,
    cols,
):
    pixels, channels = middle_ref.shape

    def read(rows):
        return middle_ref[rows, :]

    sums = finish_back(
        weights_ref.at[1], mask_ref, taps_ref, total_ref, read, table_ref, 1, cols, old_total_ref
    )
    back = norm_back(total_ref, True, sums, read, table_ref, 1, pixels, scales_ref)
    narrow = narrow_back(total_ref, middle_ref, scales_ref).astype(jnp.bfloat16)
    weight_part(act_one_ref, narrow, lanes_ref, flip_ref, columns_ref, part_ref, cols)
    sums_ref[...] = old_sums_ref[...]
    sums_ref[2:3, :] = column_total(sums[1])
    sums_ref[3:4, :] = column_total(sums[0])

    def finish(rows, carry):
        low = back(rows, rows).astype(jnp.bfloat16)
        grad_one_ref[rows, :] = low
        return carry + fold(low.astype(jnp.float32))

    zeros = jnp.zeros((8, channels), jnp.float32)
    total = zeros
    for start in range(0, pixels, CHUNK):
        total = finish(pl.ds(start, CHUNK), total)
    sums_ref[4:5, :] = column_total(total)
    keep_half(part_ref, 1, 2, keep_ref, send_ref)


def keep_half(part_ref, near, far, keep_ref, send_ref):
    me = lax.axis_index("canvas")
    rows, width = part_ref.shape[0], keep_ref.shape[1]
    for target_ref, flip in ((keep_ref, 0), (send_ref, near)):
        for slot in range(2):
            owner = me ^ flip ^ (slot * far)
            place = pl.ds(pl.multiple_of(owner * width, width), width)
            target_ref[slot * rows : (slot + 1) * rows, :] = part_ref[:, place]


def first_kernel(
    grad_one_ref,
    features_ref,
    table_ref,
    mask_ref,
    old_sums_ref,
    weights_ref,
    own_ref,
    sums_ref,
    partial_ref,
    total_ref,
    taps_ref,
    *,
    cols,
):
    def read(rows):
        return features_ref[rows, :].astype(jnp.float32)

    weights = weights_ref.at[0]
    begin_back(grad_one_ref, weights, mask_ref, taps_ref, total_ref, cols)
    sums = finish_back(weights, mask_ref, taps_ref, total_ref, read, table_ref, 0, cols)
    partial_ref[0:8, :], partial_ref[8:16, :] = sums
    sums_ref[...] = old_sums_ref[...]
    sums_ref[0:1, :] = column_total(sums[1])
    sums_ref[1:2, :] = column_total(sums[0])
    count = own_ref.shape[0]
    own = pl.ds(pl.multiple_of(lax.axis_index("height") * count, count), count)
    own_ref[...] = total_ref[own, :]


def own_kernel(
    own_ref, partial_ref, features_ref, residual_grad_ref, table_ref, input_grad_ref
):
    def read(rows):
        return features_ref[rows, :].astype(jnp.float32)

    sums = partial_ref[0:8, :], partial_ref[8:16, :]
    pixels = features_ref.shape[0]
    back = norm_back(own_ref, True, sums, read, table_ref, 0, pixels)
    count = own_ref.shape[0]
    own = pl.ds(pl.multiple_of(lax.axis_index("height") * count, count), count)
    total = residual_grad_ref[own, :] + back(own, slice(0, count))
    input_grad_ref[...] = total.astype(jnp.bfloat16)


def place_kernel(*refs):
    joints, packed_ref = refs[:-1], refs[-1]
    share = packed_ref.shape[0] // len(joints)
    me = lax.axis_index("canvas")
    for step, joint in enumerate(joints):
        place = pl.ds(pl.multiple_of((me ^ step) * share, share), share)
        packed_ref[place, :] = joint[...]


def spread_quarters(packed, flips, qkv_ref, proj_ref, qkv_hbm, proj_hbm, sems):
    quarter = packed[0].shape[0]
    inner = qkv_ref.shape[2]
    copies = []
    for index, packed_ref in enumerate(packed):
        owner = own_quarter() ^ flips[index]
        rows = pl.ds(pl.multiple_of(owner * quarter, quarter), quarter)
        qkv_ref[index] = packed_ref[:, 0:inner].astype(jnp.float32)
        proj_ref[index] = packed_ref[:, inner:].astype(jnp.float32)
        for which, (held, target) in enumerate(((qkv_ref, qkv_hbm), (proj_ref, proj_hbm))):
            copy = pltpu.make_async_copy(held.at[index], target.at[rows, :], sems.at[index, which])
            copy.start()
            copies.append(copy)
    return copies


def join_kernel(*refs):
    packed, (qkv_hbm, proj_hbm, qkv_ref, proj_ref, sems) = refs[:-5], refs[-5:]
    copies = spread_quarters(
        packed, range(len(packed)), qkv_ref, proj_ref, qkv_hbm, proj_hbm, sems
    )
    for copy in copies:
        copy.wait()


def halve_kernel(keep_ref, got_ref, hold_ref, send_ref):
    total = keep_ref[...].astype(jnp.float32) + got_ref[...].astype(jnp.float32)
    rows = hold_ref.shape[0]
    hold_ref[...] = total[0:rows]
    send_ref[0:rows, :] = total[rows:].astype(jnp.bfloat16)


def halve_sums_kernel(
    keep_one_ref,
    got_one_ref,
    keep_two_ref,
    got_two_ref,
    sums_ref,
    hold_ref,
    send_ref,
    hold_two_ref,
    send_two_ref,
):
    halve_kernel(keep_one_ref, got_one_ref, hold_ref, send_ref)
    halve_kernel(keep_two_ref, got_two_ref, hold_two_ref, send_two_ref)
    rows = hold_ref.shape[0]
    left = sums_ref[...]
    count, width = left.shape
    for part in range(2):
        low = left.astype(jnp.bfloat16)
        left = left - low.astype(jnp.float32)
        for block in range(width // LANES):
            send_ref[rows : rows + count, :] = low[:, block * LANES : (block + 1) * LANES]
            rows += count


def unpack_sums(got_ref, rows, count, width):
    total = jnp.zeros((count, width), jnp.float32)
    for part in range(2):
        blocks = []
        for block in range(width // LANES):
            blocks.append(got_ref[rows : rows + count, :].astype(jnp.float32))
            rows += count
        total = total + jnp.concatenate(blocks, axis=1)
    return total


def sums_kernel(
    sums_ref,
    near_ref,
    far_ref,
    hold_one_ref,
    got_one_ref,
    hold_two_ref,
    got_two_ref,
    share_ref,
    gains_ref,
    shifts_ref,
    conv_ref,
    qv_ref,
    bias_ref,
):
    rows = hold_one_ref.shape[0]
    for which, (hold_ref, got_ref) in enumerate(
        ((hold_one_ref, got_one_ref), (hold_two_ref, got_two_ref))
    ):
        total = hold_ref[...] + got_ref[0:rows, :].astype(jnp.float32)
        share_ref[which] = total.reshape(share_ref.shape[1:])
    total = sums_ref[...] + near_ref[...] + far_ref[...]
    total = total + unpack_sums(got_one_ref, rows, *total.shape)
    for row, start in enumerate((0, 2, 5)):
        gains_ref[row : row + 1, :] = total[start : start + 1]
        shifts_ref[row : row + 1, :] = total[start + 1 : start + 2]
    conv_ref[0:1, :] = total[4:5]
    conv_ref[1:2, :] = total[7:8]
    qv_ref[...] = total[8:10]
    bias_ref[...] = total[10:11]


def call_kernel(kernel, outputs, scratch, operands, places, flops, limit, out_places=None, aliases={}):
    out_places = out_places or "v" * len(outputs)
    spaces = {
        "v": pl.BlockSpec(memory_space=pltpu.VMEM),
        "s": pl.BlockSpec(memory_space=pltpu.SMEM),
        "h": pl.BlockSpec(memory_space=pl.ANY),
        "o": pl.BlockSpec(memory_space=pltpu.VMEM),
        "a": pl.BlockSpec(memory_space=pl.ANY),
    }
    moved = 8 * flops // LANES
    held = {"v": pltpu.VMEM, "h": pltpu.HBM, "o": jax.ShapeDtypeStruct}
    operands = [
        pltpu.with_memory_space_constraint(array, pltpu.HBM) if place == "h" else array
        for array, place in zip(operands, places)
    ]
    return pl.pallas_call(
        kernel,
        out_shape=[held[place](*output) for output, place in zip(outputs, out_places)],
        in_specs=[spaces[place] for place in places],
        out_specs=[spaces[place] for place in out_places],
        scratch_shapes=scratch,
        input_output_aliases=aliases,
        compiler_params=pltpu.CompilerParams(vmem_limit_bytes=limit * 2**20),
        cost_estimate=pl.CostEstimate(flops=flops, bytes_accessed=moved, transcendentals=0),
    )(*operands)


def send_height(block, step):
    size = lax.axis_size("height")
    return lax.ppermute(block, "height", [(i, i ^ step) for i in range(size)])


def with_cores(blocks):
    return [piece for block in blocks for piece in (block, send_height(block, 1))]


def send_canvas(block, step):
    size = lax.axis_size("canvas")
    return lax.ppermute(block, "canvas", [(i, i ^ step) for i in range(size)])


def trade_canvas(pieces):
    return [pieces[0]] + [send_canvas(piece, step) for step, piece in enumerate(pieces) if step]


def whole_canvas(
    features,
    tile_ids,
    norm_gains,
    norm_shifts,
    conv_weights,
    conv_biases,
    qkv_weight,
    qv_bias,
    proj_weight,
    proj_bias,
    cotangent,
):
    height_size = lax.axis_size("height")
    canvas_size = lax.axis_size("canvas")
    local_rows, cols, channels = features.shape[1:]
    all_rows = tile_ids.shape[1]
    pixels = all_rows * cols
    own_pixels = local_rows * cols
    out_share = channels // height_size
    ci_share = channels // canvas_size
    quarter = channels // 4
    row_share = quarter // canvas_size
    low, wide = jnp.bfloat16, jnp.float32

    own_features = features.reshape(own_pixels, channels)
    own_grad = cotangent.reshape(own_pixels, channels)
    steps = range(2, height_size, 2)
    held_features = [own_features] + [send_height(own_features, step) for step in steps]
    plane = ((pixels, channels), low)
    plane_wide = ((pixels, channels), wide)
    sums_shape = ((16, channels), wide)
    mixed_shapes = [((row_share, 4 * channels), low)] * canvas_size
    taps = pltpu.VMEM((pixels + 2 * cols, 3 * channels), low)
    held_wide = pltpu.VMEM((pixels, channels), wide)
    flipped = pltpu.VMEM((channels, pixels), low)
    narrow = pltpu.VMEM((NARROW, pixels), low)
    columns = pltpu.VMEM((9 * out_share, pixels), low)
    part_held = pltpu.VMEM((9 * out_share, channels), low)
    sem = pltpu.SemaphoreType.DMA
    conv_flops = 2 * 9 * pixels * channels * channels
    dot_flops = 2 * pixels * channels * channels
    score_flops = 2 * pixels * pixels * channels
    scale = channels ** (-0.5)

    (
        held_conv,
        turned,
        held_qkv,
        held_proj,
        params,
        mask,
        lane_mask,
        id_rows,
        id_cols,
    ) = call_kernel(
        functools.partial(hold_kernel, cols=cols),
        [
            (conv_weights.shape, low),
            ((2, 3, channels, 3 * channels), low),
            (qkv_weight.shape, low),
            (proj_weight.shape, low),
            ((24, channels), wide),
            ((2, pixels, LANES), wide),
            ((8, pixels), wide),
            ((pixels, LANES), jnp.int32),
            ((8, pixels), jnp.int32),
        ],
        [
            pltpu.SMEM(tile_ids.shape, jnp.int32),
            pltpu.VMEM(norm_gains.shape, wide),
            pltpu.VMEM(norm_shifts.shape, wide),
            pltpu.VMEM(conv_biases.shape, wide),
            pltpu.VMEM(qv_bias.shape, wide),
            pltpu.VMEM((1, channels), wide),
            sem((27,)),
        ],
        [
            tile_ids,
            norm_gains,
            norm_shifts,
            conv_biases,
            conv_weights,
            qkv_weight,
            proj_weight,
            qv_bias,
            proj_bias.reshape(1, channels),
        ],
        "h" * 9,
        conv_flops,
        8,
    )
    held_features[1:] = [
        lax.optimization_barrier((params, block))[1] for block in held_features[1:]
    ]
    pieces = with_cores(held_features)
    far_grad, *pieces[4::2] = lax.optimization_barrier((own_grad, *held_features[2:]))
    held_grads = [own_grad, send_height(own_grad, 2)]
    held_grads[1], pieces[2] = lax.optimization_barrier((held_grads[1], held_features[1]))
    held_grads += [send_height(far_grad, step) for step in steps[1:]]

    all_features, act_one, middle, act_two, residual, table = call_kernel(
        functools.partial(conv_kernel, cols=cols, count=height_size),
        [plane, plane, plane_wide, plane, plane_wide, ((24, channels), wide)],
        [pltpu.VMEM((own_pixels, channels), low), taps, sem],
        [*pieces, held_conv, params, mask],
        "h" + "v" * (height_size + 2),
        2 * conv_flops,
        16,
    )
    residual, *held_grads = lax.optimization_barrier((residual, *held_grads))
    grad_pieces = with_cores(held_grads)
    normed, query, key, value, soft, out_flip, output = call_kernel(
        functools.partial(score_kernel, score_scale=scale),
        [
            plane,
            plane,
            plane,
            plane,
            ((pixels, pixels), low),
            ((channels, pixels), low),
            ((own_pixels, channels), low),
        ],
        [
            flipped,
            *[pltpu.VMEM((pixels, SCORE_ROWS), wide)] * (pixels // SCORE_ROWS),
        ],
        [
            held_qkv,
            held_proj,
            residual,
            table,
            id_rows,
            id_cols,
        ],
        "vvvvvv",
        3 * dot_flops + 2 * score_flops,
        20,
        "v" * 6 + "o",
    )
    normed, *grad_pieces = lax.optimization_barrier((normed, *grad_pieces))
    all_grad, packed, sums, *mixed = call_kernel(
        functools.partial(attention_kernel, score_scale=scale, count=height_size),
        [plane, ((pixels, 3 * channels), low), sums_shape, *mixed_shapes],
        [
            pltpu.VMEM((quarter, 4 * channels), low),
            flipped,
            pltpu.VMEM((pixels, channels), low),
            pltpu.VMEM((pixels, pixels), low),
            pltpu.VMEM((quarter, pixels), low),
            sem((height_size,)),
            *[pltpu.VMEM((pixels, SCORE_ROWS), wide)] * (pixels // SCORE_ROWS),
        ],
        [held_proj, normed, query, key, value, soft, out_flip, *grad_pieces],
        "vvvvvvvh" + "a" * (height_size - 1),
        3 * dot_flops + 4 * score_flops,
        20,
    )
    mixed = trade_canvas(mixed)
    halves = [((18 * out_share, ci_share), low)] * 2
    residual_grad, grad_two, sums, keep_two, send_two = call_kernel(
        functools.partial(third_kernel, cols=cols),
        [plane_wide, plane, sums_shape, *halves],
        [held_wide, narrow, columns, part_held, pltpu.VMEM((8, channels), wide)],
        [held_qkv, all_grad, packed, residual, table, act_two, lane_mask, sums],
        "vvvvvvvv",
        3 * dot_flops + conv_flops // height_size,
        16,
    )
    half_total, half_taps = call_kernel(
        functools.partial(turn_kernel, cols=cols),
        [plane_wide, (taps.shape, low)],
        [],
        [grad_two, mask, turned],
        "vvv",
        2 * conv_flops // 3,
        16,
    )
    half_total, *mixed = lax.optimization_barrier((half_total, *mixed))
    mixed_sum = mixed[0].astype(wide)
    for piece in mixed[1:]:
        mixed_sum = mixed_sum + piece.astype(wide)
    joints = trade_canvas([mixed_sum.astype(low)] * canvas_size)
    grad_one, sums, keep_one, send_one = call_kernel(
        functools.partial(second_kernel, cols=cols),
        [plane, sums_shape, *halves],
        [held_wide, narrow, columns, part_held, pltpu.VMEM((8, channels), wide)],
        [half_total, half_taps, middle, table, act_one, mask, lane_mask, turned, sums],
        "vvvvvvvvv",
        conv_flops // 2,
        20,
    )
    grad_one, *joints = lax.optimization_barrier((grad_one, *joints))
    (own_mixed,) = call_kernel(
        place_kernel,
        [((quarter, 4 * channels), low)],
        [],
        joints,
        "v" * canvas_size,
        1,
        12,
    )
    own_mixed, send_one, send_two = lax.optimization_barrier((own_mixed, send_one, send_two))
    chip_mixed = send_height(own_mixed, 2)
    core_mixed = send_height(own_mixed, 1)
    got_one, got_two = send_canvas(send_one, 1), send_canvas(send_two, 2)
    own_total, sums, partial_sums = call_kernel(
        functools.partial(first_kernel, cols=cols),
        [((own_pixels, channels), wide), sums_shape, sums_shape],
        [held_wide, taps],
        [grad_one, all_features, table, mask, sums, turned],
        "vvvvvv",
        1,
        20,
    )
    share_rows = 9 * out_share
    send_rows = share_rows + 2 * sums_shape[0][0] * channels // LANES
    sums, core_mixed, got_one, got_two = lax.optimization_barrier(
        (sums, core_mixed, got_one, got_two)
    )
    hold_one, send_one, hold_two, send_two = call_kernel(
        halve_sums_kernel,
        [
            ((share_rows, ci_share), wide),
            ((send_rows, ci_share), low),
            ((share_rows, ci_share), wide),
            ((share_rows, ci_share), low),
        ],
        [],
        [keep_one, got_one, keep_two, got_two, sums],
        "vvvvv",
        1,
        12,
    )
    got_two = send_canvas(send_two, 1)
    got_one = send_canvas(send_one, 2)
    near_sums, far_sums = send_canvas(sums, 1), send_canvas(sums, 3)
    chip_mixed, hold_one = lax.optimization_barrier((chip_mixed, hold_one))
    both_mixed = send_height(chip_mixed, 1)
    own_total, hold_one = lax.optimization_barrier((own_total, hold_one))
    (input_grad,) = call_kernel(
        own_kernel,
        [((own_pixels, channels), low)],
        [],
        [own_total, partial_sums, all_features, residual_grad, table],
        "vvvvv",
        dot_flops // 4,
        12,
        "o",
    )
    input_grad, both_mixed = lax.optimization_barrier((input_grad, both_mixed))
    qkv_grad, proj_grad = call_kernel(
        join_kernel,
        [(qkv_weight.shape, wide), (proj_weight.shape, wide)],
        [
            pltpu.VMEM((4, quarter, 3 * channels), wide),
            pltpu.VMEM((4, quarter, channels), wide),
            sem((4, 2)),
        ],
        [own_mixed, chip_mixed, core_mixed, both_mixed],
        "vvvv",
        1,
        12,
        "hh",
    )
    qkv_grad, got_one, got_two, near_sums, far_sums = lax.optimization_barrier(
        (qkv_grad, got_one, got_two, near_sums, far_sums)
    )
    vector_shapes = [norm_gains.shape, norm_shifts.shape, conv_biases.shape, qv_bias.shape]
    conv_grad, gains_grad, shifts_grad, biases_grad, qv_grad, proj_bias_grad = call_kernel(
        sums_kernel,
        [((2, 3, 3, out_share, ci_share), wide)]
        + [(shape, wide) for shape in vector_shapes + [(1, channels)]],
        [],
        [sums, near_sums, far_sums, hold_one, got_one, hold_two, got_two],
        "vvvvvvv",
        1,
        12,
        "o" * 6,
    )
    own_shape = (1, local_rows, cols, channels)
    return (
        output.reshape(own_shape),
        input_grad.reshape(own_shape),
        gains_grad,
        shifts_grad,
        jnp.swapaxes(conv_grad, 3, 4),
        biases_grad,
        qkv_grad,
        qv_grad,
        proj_grad,
        proj_bias_grad.reshape(channels),
    )


def on_device(*arrays):
    features, tile_ids = arrays[0], arrays[1]
    local_rows, cols, channels = features.shape[1:]
    pixels = tile_ids.shape[1] * cols
    height_size, canvas_size = lax.axis_size("height"), lax.axis_size("canvas")
    powers = all(size & (size - 1) == 0 for size in (height_size, canvas_size, cols))
    fits = (
        powers
        and height_size > 2
        and canvas_size == 4
        and channels == LANES * canvas_size
        and pixels <= MOST_PIXELS
        and pixels % FILL_ROWS == 0
        and FILL_ROWS % CHUNK == 0
        and pixels % SCORE_ROWS == 0
        and pixels % KEY_ROWS == 0
        and (local_rows * cols) % LANES == 0
        and CHUNK % cols == 0
        and cols % 16 == 0
        and channels % (LANES * canvas_size) == 0
        and 2 * channels == NARROW * height_size
    )
    return whole_canvas(*arrays) if fits else split_canvas(*arrays)


def solution(mesh):
    in_specs = (
        P("canvas", "height", None, None),
        P("canvas", None),
        P(),
        P(),
        P(),
        P(),
        P(),
        P(),
        P(),
        P(),
        P("canvas", "height", None, None),
    )
    out_specs = (
        P("canvas", "height", None, None),
        P("canvas", "height", None, None),
        P(),
        P(),
        P(None, None, None, "canvas", "height"),
        P(),
        P(),
        P(),
        P(),
        P(),
    )
    return jax.shard_map(
        on_device, mesh=mesh, in_specs=in_specs, out_specs=out_specs, check_vma=False
    )
```

```python
import functools

import jax
import jax.numpy as jnp
from jax import lax
from jax.experimental import pallas as pl
from jax.experimental.pallas import tpu as pltpu
from jax.sharding import PartitionSpec as P

GROUPS = 32


epsilon = 1e-06
masked_score = -1e30
MOST_PIXELS = 1024
LANES = 128
NARROW = 128
CHUNK = 128
FILL_ROWS = 256
QUERY_ROWS = 512
SCORE_ROWS = 256
KEY_ROWS = 256


def extended(block, sides, width):
    for axis, dim in sides:
        count = lax.axis_size(axis)
        forward = [(i, i + 1) for i in range(count - 1)]
        backward = [(target, source) for source, target in forward]
        low = lax.ppermute(
            lax.slice_in_dim(block, block.shape[dim] - width, None, axis=dim), axis, forward
        )
        high = lax.ppermute(lax.slice_in_dim(block, 0, width, axis=dim), axis, backward)
        block = jnp.concatenate([low, block, high], axis=dim)
    return block


def group_total(vector):
    return vector.reshape(GROUPS, -1).sum(axis=1)


def spread_groups(vector, channels):
    return jnp.repeat(vector, channels // GROUPS)


def norm_forward(values, gain, shift, members):
    channels = values.shape[1]
    totals = lax.psum(group_total(jnp.sum(values, axis=0)), "height")
    centered = values - spread_groups(totals / members, channels)
    squares = lax.psum(group_total(jnp.sum(centered * centered, axis=0)), "height")
    inverse = spread_groups(lax.rsqrt(squares / members + epsilon), channels)
    normed = centered * inverse
    return (normed, inverse, normed * gain + shift)


def norm_backward(grad_in, normed, inverse, gain, members):
    channels = grad_in.shape[1]
    scaled = grad_in * gain
    both_sums = lax.psum(
        (group_total(jnp.sum(scaled, axis=0)), group_total(jnp.sum(scaled * normed, axis=0))),
        "height",
    )
    mean_grad = spread_groups(both_sums[0] / members, channels)
    mean_cross = spread_groups(both_sums[1] / members, channels)
    result = inverse * (scaled - mean_grad - normed * mean_cross)
    return (result, jnp.sum(grad_in * normed, axis=0), jnp.sum(grad_in, axis=0))


def swish(values):
    return values * jax.nn.sigmoid(values)


def swish_slope(values):
    sigmoid_part = jax.nn.sigmoid(values)
    return sigmoid_part * (1.0 + values * (1.0 - sigmoid_part))


def tap_columns(padded, row_mask, local_rows, canvas_cols):
    pieces = []
    for row_tap in range(3):
        rows_taken = padded[row_tap : row_tap + local_rows] * row_mask[:, row_tap, None, None]
        for col_tap in range(3):
            pieces.append(rows_taken[:, col_tap : col_tap + canvas_cols])
    stacked = jnp.concatenate(pieces, axis=2)
    return stacked.reshape(local_rows * canvas_cols, stacked.shape[2])


def conv_forward(acts, row_mask, weight, bias):
    local_rows, canvas_cols, channels = acts.shape
    rimmed = extended(acts, (("height", 0),), 1)
    padded = jnp.pad(rimmed, ((0, 0), (1, 1), (0, 0)))
    gathered = tap_columns(padded, row_mask, local_rows, canvas_cols)
    result = (
        jnp.dot(
            gathered, weight.reshape(9 * channels, channels), preferred_element_type=jnp.float32
        )
        + bias
    )
    return (result, gathered)


def conv_backward(grad_low, row_mask, weight, gathered):
    local_rows, canvas_cols, channels = grad_low.shape
    flat_grad = grad_low.reshape(local_rows * canvas_cols, channels)
    weight_grad = lax.dot_general(
        gathered, flat_grad, (((0,), (0,)), ((), ())), preferred_element_type=jnp.float32
    )
    rimmed = extended(grad_low, (("height", 0),), 1)
    padded = jnp.pad(rimmed, ((0, 0), (1, 1), (0, 0)))
    grad_taps = tap_columns(padded, row_mask, local_rows, canvas_cols)
    flipped = jnp.transpose(weight[::-1, ::-1], (0, 1, 3, 2)).reshape(9 * channels, channels)
    input_part = jnp.dot(grad_taps, flipped, preferred_element_type=jnp.float32)
    return (
        input_part,
        weight_grad.reshape(3, 3, channels, channels),
        jnp.sum(flat_grad.astype(jnp.float32), axis=0),
    )


def take_rows(array, offset, count):
    return lax.dynamic_slice_in_dim(array, offset, count)


def score_grads(
    queries, out_grad, log_total, row_dots, query_ids, key_rows, value_rows, key_ids, score_scale
):
    scores = (
        lax.dot_general(
            queries, key_rows, (((1,), (1,)), ((), ())), preferred_element_type=jnp.float32
        )
        * score_scale
    )
    same_tile = query_ids[:, None] == key_ids[None, :]
    softmax_block = jnp.exp(jnp.where(same_tile, scores - log_total[:, None], masked_score))
    weight_grad = lax.dot_general(
        out_grad, value_rows, (((1,), (1,)), ((), ())), preferred_element_type=jnp.float32
    )
    score_grad = (softmax_block * (weight_grad - row_dots[:, None])).astype(jnp.bfloat16)
    return (softmax_block.astype(jnp.bfloat16), score_grad)


def split_canvas(
    features,
    tile_ids,
    norm_gains,
    norm_shifts,
    conv_weights,
    conv_biases,
    qkv_weight,
    qv_bias,
    proj_weight,
    proj_bias,
    cotangent,
):
    height_size = lax.axis_size("height")
    local_rows = features.shape[1]
    canvas_cols = features.shape[2]
    channels = features.shape[3]
    pixels = local_rows * canvas_cols
    row_ids = tile_ids[0]
    all_rows = row_ids.shape[0]
    members = float(all_rows * canvas_cols * (channels // GROUPS))
    score_scale = channels ** (-0.5)
    first_row = lax.axis_index("height") * local_rows
    edge_ids = jnp.full((1,), -1, jnp.int32)
    padded_ids = jnp.concatenate([edge_ids, row_ids, edge_ids])
    near_ids = lax.dynamic_slice_in_dim(padded_ids, first_row, local_rows + 2)
    own_rows = near_ids[1 : local_rows + 1]
    row_mask = jnp.stack(
        [near_ids[row_tap : row_tap + local_rows] == own_rows for row_tap in range(3)], axis=1
    ).astype(jnp.bfloat16)
    key_ids = jnp.repeat(row_ids, canvas_cols)
    query_ids = jnp.repeat(own_rows, canvas_cols)
    grid_shape = (local_rows, canvas_cols, channels)
    inputs = features[0].reshape(pixels, channels).astype(jnp.float32)
    normed_one, inverse_one, pre_one = norm_forward(inputs, norm_gains[0], norm_shifts[0], members)
    act_one = swish(pre_one).astype(jnp.bfloat16).reshape(grid_shape)
    middle, taps_one = conv_forward(act_one, row_mask, conv_weights[0], conv_biases[0])
    normed_two, inverse_two, pre_two = norm_forward(middle, norm_gains[1], norm_shifts[1], members)
    act_two = swish(pre_two).astype(jnp.bfloat16).reshape(grid_shape)
    branch, taps_two = conv_forward(act_two, row_mask, conv_weights[1], conv_biases[1])
    residual = inputs + branch
    normed_three, inverse_three, pre_three = norm_forward(
        residual, norm_gains[2], norm_shifts[2], members
    )
    attn_input = pre_three.astype(jnp.bfloat16)
    mixed = jnp.dot(attn_input, qkv_weight, preferred_element_type=jnp.float32)
    queries = (mixed[:, :channels] + qv_bias[0]).astype(jnp.bfloat16)
    key_rows = mixed[:, channels : 2 * channels].astype(jnp.bfloat16)
    value_rows = (mixed[:, 2 * channels :] + qv_bias[1]).astype(jnp.bfloat16)
    running_max = jnp.full((pixels,), masked_score, jnp.float32)
    key_piece = lax.all_gather(key_rows, "height", axis=0, tiled=True)
    value_piece = lax.all_gather(value_rows, "height", axis=0, tiled=True)
    scores = (
        lax.dot_general(
            queries, key_piece, (((1,), (1,)), ((), ())), preferred_element_type=jnp.float32
        )
        * score_scale
    )
    same_tile = query_ids[:, None] == key_ids[None, :]
    scores = jnp.where(same_tile, scores, masked_score)
    new_max = jnp.maximum(running_max, jnp.max(scores, axis=1))
    weights = jnp.where(same_tile, jnp.exp(scores - new_max[:, None]), 0.0)
    summed_out = jnp.dot(
        weights.astype(jnp.bfloat16), value_piece, preferred_element_type=jnp.float32
    )
    total_weight = jnp.sum(weights, axis=1)
    log_total = new_max + jnp.log(total_weight)
    attended = summed_out / total_weight[:, None]
    attended_low = attended.astype(jnp.bfloat16)
    output = (
        residual
        + jnp.dot(attended_low, proj_weight, preferred_element_type=jnp.float32)
        + proj_bias
    )
    out_grad = cotangent[0].reshape(pixels, channels)
    out_grad_full = out_grad.astype(jnp.float32)
    proj_grad = lax.dot_general(
        attended_low, out_grad, (((0,), (0,)), ((), ())), preferred_element_type=jnp.float32
    )
    proj_bias_grad = jnp.sum(out_grad_full, axis=0)
    attended_grad = lax.dot_general(
        out_grad, proj_weight, (((1,), (1,)), ((), ())), preferred_element_type=jnp.float32
    ).astype(jnp.bfloat16)
    row_dots = jnp.sum(attended_grad.astype(jnp.float32) * attended, axis=1)
    block_rows = pixels * min(height_size, 8)
    zero_block = jnp.zeros((pixels, channels), jnp.float32)
    key_all, value_all = (
        lax.all_gather(key_rows, "height", axis=0, tiled=True),
        lax.all_gather(value_rows, "height", axis=0, tiled=True),
    )
    query_all, grad_all = (
        lax.all_gather(queries, "height", axis=0, tiled=True),
        lax.all_gather(attended_grad, "height", axis=0, tiled=True),
    )
    total_all, dots_all = (
        lax.all_gather(log_total, "height", axis=0, tiled=True),
        lax.all_gather(row_dots, "height", axis=0, tiled=True),
    )

    def own_query_step(running, block_index):
        offset = block_index * block_rows
        key_part = take_rows(key_all, offset, block_rows)
        rounded, score_grad = score_grads(
            queries,
            attended_grad,
            log_total,
            row_dots,
            query_ids,
            key_part,
            take_rows(value_all, offset, block_rows),
            take_rows(key_ids, offset, block_rows),
            score_scale,
        )
        return (
            running
            + jnp.dot(score_grad, key_part, preferred_element_type=jnp.float32) * score_scale,
            None,
        )

    def own_key_step(running, block_index):
        offset = block_index * block_rows
        query_part = take_rows(query_all, offset, block_rows)
        grad_part = take_rows(grad_all, offset, block_rows)
        rounded, score_grad = score_grads(
            query_part,
            grad_part,
            take_rows(total_all, offset, block_rows),
            take_rows(dots_all, offset, block_rows),
            take_rows(key_ids, offset, block_rows),
            key_rows,
            value_rows,
            query_ids,
            score_scale,
        )
        key_part = (
            lax.dot_general(
                score_grad, query_part, (((0,), (0,)), ((), ())), preferred_element_type=jnp.float32
            )
            * score_scale
        )
        value_part = lax.dot_general(
            rounded, grad_part, (((0,), (0,)), ((), ())), preferred_element_type=jnp.float32
        )
        return ((running[0] + key_part, running[1] + value_part), None)

    block_count = key_all.shape[0] // block_rows
    query_grad, unused_one = lax.scan(own_query_step, zero_block, jnp.arange(block_count))
    (key_grad, value_grad), unused_two = lax.scan(
        own_key_step, (zero_block, zero_block), jnp.arange(block_count)
    )
    query_low = query_grad.astype(jnp.bfloat16)
    key_low = key_grad.astype(jnp.bfloat16)
    value_low = value_grad.astype(jnp.bfloat16)
    stacked_grad = jnp.concatenate([query_low, key_low, value_low], axis=1)
    qkv_grad = lax.dot_general(
        attn_input, stacked_grad, (((0,), (0,)), ((), ())), preferred_element_type=jnp.float32
    )
    qv_grad = jnp.stack(
        [
            jnp.sum(query_low.astype(jnp.float32), axis=0),
            jnp.sum(value_low.astype(jnp.float32), axis=0),
        ]
    )
    normed_grad = lax.dot_general(
        stacked_grad, qkv_weight, (((1,), (1,)), ((), ())), preferred_element_type=jnp.float32
    )
    back_three, gain_three, shift_three = norm_backward(
        normed_grad, normed_three, inverse_three, norm_gains[2], members
    )
    residual_grad = out_grad_full + back_three
    grad_two = residual_grad.astype(jnp.bfloat16).reshape(grid_shape)
    act_two_grad, weight_two_grad, bias_two_grad = conv_backward(
        grad_two, row_mask, conv_weights[1], taps_two
    )
    middle_grad, gain_two, shift_two = norm_backward(
        act_two_grad * swish_slope(pre_two), normed_two, inverse_two, norm_gains[1], members
    )
    grad_one = middle_grad.astype(jnp.bfloat16).reshape(grid_shape)
    act_one_grad, weight_one_grad, bias_one_grad = conv_backward(
        grad_one, row_mask, conv_weights[0], taps_one
    )
    input_back, gain_one, shift_one = norm_backward(
        act_one_grad * swish_slope(pre_one), normed_one, inverse_one, norm_gains[0], members
    )
    input_grad = residual_grad + input_back
    conv_grad = jnp.stack([weight_one_grad, weight_two_grad])
    conv_part = lax.psum_scatter(conv_grad, "height", scatter_dimension=4, tiled=True)
    conv_part = lax.psum_scatter(
        conv_part.astype(jnp.bfloat16), "canvas", scatter_dimension=3, tiled=True
    ).astype(jnp.float32)
    summed = lax.psum(
        (
            jnp.stack([gain_one, gain_two, gain_three]),
            jnp.stack([shift_one, shift_two, shift_three]),
            jnp.stack([bias_one_grad, bias_two_grad]),
            qkv_grad,
            qv_grad,
            proj_grad,
            proj_bias_grad,
        ),
        ("canvas", "height"),
    )
    return (
        output.astype(jnp.bfloat16).reshape((1,) + grid_shape),
        input_grad.astype(jnp.bfloat16).reshape((1,) + grid_shape),
        summed[0],
        summed[1],
        conv_part,
        summed[2],
        summed[3],
        summed[4],
        summed[5],
        summed[6],
    )


def fold(block):
    rows, width = block.shape
    return jnp.sum(block.reshape(rows // 8, 8, width), axis=0)


def group_lanes(block, group):
    lane = lax.broadcasted_iota(jnp.int32, block.shape, 1)
    width = block.shape[1]
    step = 1
    while step < group:
        above = pltpu.roll(block, step, 1)
        below = pltpu.roll(block, width - step, 1)
        block = block + jnp.where((lane & step) != 0, above, below)
        step *= 2
    return block


def group_mean(partial, members):
    spread = group_lanes(partial, partial.shape[1] // GROUPS)
    return jnp.sum(spread, axis=0, keepdims=True) * (1.0 / members)


def widen(block, width):
    return jnp.concatenate([block] * (width // block.shape[1]), axis=1)


def each_block(pixels, block, body, carry=0):
    def step(index, carry):
        return body(pl.ds(pl.multiple_of(index * block, block), block), carry)

    return lax.fori_loop(0, pixels // block, step, carry)


def each_chunk(pixels, body, carry):
    return each_block(pixels, CHUNK, body, carry)


def aligned(start, step):
    return start if isinstance(start, int) else pl.multiple_of(start, step)


class RunningStats:
    def __init__(self, channels):
        self.width = channels // GROUPS
        self.reference = None
        self.sums = self.squares = jnp.zeros((8, channels), jnp.float32)

    def add(self, block):
        if self.reference is None:
            self.reference = group_mean(block[0:8], 8.0 * self.width)
        offset = block - self.reference
        self.sums = self.sums + fold(offset)
        self.squares = self.squares + fold(offset * offset)

    def finish(self, pixels):
        both = group_lanes(jnp.concatenate([self.sums, self.squares], axis=0), self.width)
        share = 1.0 / (pixels * self.width)
        offset = column_total(both[0:8]) * share
        variance = column_total(both[8:16]) * share - offset * offset
        return self.reference + offset, lax.rsqrt(jnp.maximum(variance, 0.0) + epsilon)


def put_taps(taps_ref, block, rows, cols):
    count, channels = block.shape
    place = lax.broadcasted_iota(jnp.int32, block.shape, 0) & (cols - 1)
    left = jnp.where(place == 0, 0.0, pltpu.roll(block, 1, 0))
    right = jnp.where(place == cols - 1, 0.0, pltpu.roll(block, count - 1, 0))
    inner = pl.ds(aligned(rows.start + cols, cols), count)
    taps_ref[inner, 0:channels] = left.astype(jnp.bfloat16)
    taps_ref[inner, channels : 2 * channels] = block.astype(jnp.bfloat16)
    taps_ref[inner, 2 * channels :] = right.astype(jnp.bfloat16)


def clear_edges(taps_ref, cols):
    edge = jnp.zeros((cols, taps_ref.shape[1]), taps_ref.dtype)
    taps_ref[0:cols, :] = edge
    taps_ref[taps_ref.shape[0] - cols :, :] = edge


def begin_conv(taps_ref, product, total_ref, fill, first, cols):
    for start in range(0, total_ref.shape[0], FILL_ROWS):
        for inner in range(start, start + FILL_ROWS, CHUNK):
            fill(pl.ds(inner, CHUNK))
        rows = pl.ds(start, FILL_ROWS)
        total_ref[rows, :] = first(rows, product(taps_ref, pl.ds(start + cols, FILL_ROWS), 1))


def add_rows(taps_ref, product, mask_ref, total_ref, row_tap, last, cols, old_ref=None):
    pixels, channels = total_ref.shape
    old_ref = total_ref if old_ref is None else old_ref

    def step(rows, shifted):
        part = product(taps_ref, shifted, row_tap)
        mask = widen(mask_ref[row_tap // 2, rows, :], channels)
        value = old_ref[rows, :] + mask * part
        total_ref[rows, :] = value if last is None else last(rows, value)

    if last is None:

        def add(rows, carry):
            start = pl.multiple_of(rows.start + row_tap * cols, cols)
            step(rows, pl.ds(start, FILL_ROWS))
            return carry

        each_block(pixels, FILL_ROWS, add)
        return
    for start in range(0, pixels, FILL_ROWS):
        step(pl.ds(start, FILL_ROWS), pl.ds(start + row_tap * cols, FILL_ROWS))


def run_conv(taps_ref, product, mask_ref, total_ref, fill, first, last, cols):
    begin_conv(taps_ref, product, total_ref, fill, first, cols)
    add_rows(taps_ref, product, mask_ref, total_ref, 0, None, cols)
    add_rows(taps_ref, product, mask_ref, total_ref, 2, last, cols)


def product_forward(weight_ref):
    channels = weight_ref.shape[-1]

    def product(taps_ref, shifted, row_tap):
        return jnp.dot(
            taps_ref[shifted, :],
            weight_ref[row_tap].reshape(3 * channels, channels),
            preferred_element_type=jnp.float32,
        )

    return product


def product_backward(weight_ref):
    def product(taps_ref, shifted, row_tap):
        return lax.dot_general(
            taps_ref[shifted, :],
            weight_ref[row_tap],
            (((1,), (1,)), ((), ())),
            preferred_element_type=jnp.float32,
        )

    return product


def activation(read, mean, inverse, gain, shift, act_ref, taps_ref, cols):
    scale, offset = 0.5 * inverse * gain, 0.5 * shift

    def fill(rows):
        half = (read(rows) - mean) * scale + offset
        act = half * (1.0 + jnp.tanh(half))
        act_ref[rows, :] = act.astype(jnp.bfloat16)
        put_taps(taps_ref, act, rows, cols)

    return fill


def back_means(sums, gain, pixels):
    channels = gain.shape[1]
    members = float(pixels * (channels // GROUPS))
    return group_mean(sums[0] * gain, members), group_mean(sums[1] * gain, members)


def column_total(partial):
    return jnp.sum(partial, axis=0, keepdims=True)


def weight_part(act_ref, narrow, lanes_ref, flip_ref, columns_ref, part_ref, cols):
    pixels, channels = act_ref.shape
    height = lax.axis_index("height")
    share = NARROW // 2
    flip_ref[...] = narrow.T
    own = pl.ds(pl.multiple_of((height % 2) * share, share), share)
    grad = flip_ref[own, :].astype(jnp.float32)
    column = lax.broadcasted_iota(jnp.int32, grad.shape, 1) & (cols - 1)
    for col_tap in range(3):
        shifted = grad
        if col_tap == 0:
            shifted = jnp.where(column == cols - 1, 0.0, pltpu.roll(grad, pixels - 1, 1))
        elif col_tap == 2:
            shifted = jnp.where(column == 0, 0.0, pltpu.roll(grad, 1, 1))
        for row_tap in range(3):
            tap = 3 * row_tap + col_tap
            place = slice(tap * share, (tap + 1) * share)
            if row_tap == 1:
                columns_ref[place, :] = shifted.astype(jnp.bfloat16)
                continue
            side, turn = (0, pixels - cols) if row_tap == 0 else (1, cols)
            masked = (shifted * lanes_ref[side : side + 1, :]).astype(jnp.bfloat16)
            columns_ref[place, :] = pltpu.roll(masked, turn, 1)
    part_ref[...] = jnp.dot(
        columns_ref[...], act_ref[...], preferred_element_type=jnp.float32
    ).astype(jnp.bfloat16)


def begin_back(grad_ref, weights_ref, mask_ref, taps_ref, total_ref, cols):
    clear_edges(taps_ref, cols)

    def fill(rows):
        put_taps(taps_ref, grad_ref[rows, :].astype(jnp.float32), rows, cols)

    product = product_backward(weights_ref)
    begin_conv(taps_ref, product, total_ref, fill, lambda rows, part: part, cols)
    add_rows(taps_ref, product, mask_ref, total_ref, 0, None, cols)


def finish_back(
    weights_ref, mask_ref, taps_ref, total_ref, read, table_ref, which, cols, old_ref=None
):
    mean, inverse, gain, shift = norm_rows(table_ref, which)
    scale, offset = 0.5 * inverse * gain, 0.5 * shift
    sums = []

    def slope(rows, value):
        centered = read(rows) - mean
        half = centered * scale + offset
        turn = jnp.tanh(half)
        double = value * ((1.0 + turn) * (1.0 + half * (1.0 - turn)))
        sums.append((fold(double), fold(double * centered)))
        return double

    add_rows(
        taps_ref, product_backward(weights_ref), mask_ref, total_ref, 2, slope, cols, old_ref
    )
    plain, cross = sum(pair[0] for pair in sums), sum(pair[1] for pair in sums)
    return 0.5 * plain, 0.5 * inverse * cross


def norm_back(total_ref, double, sums, read, table_ref, which, pixels, scales_ref=None):
    mean, inverse, gain, shift = norm_rows(table_ref, which)
    mean_grad, mean_cross = back_means(sums, gain, pixels)
    slope = inverse * gain * (0.5 if double else 1.0)
    level, tilt = inverse * mean_grad, inverse * inverse * mean_cross
    if scales_ref is not None:
        for row, scales in enumerate((mean, slope, level, tilt)):
            scales_ref[row : row + 1, :] = scales

    def back(rows, inner):
        return total_ref[inner, :] * slope - level - (read(rows) - mean) * tilt

    return back


def own_lanes():
    block = lax.axis_index("height") // 2
    return pl.ds(pl.multiple_of(block * NARROW, NARROW), NARROW)


def narrow_back(total_ref, value_ref, scales_ref):
    lanes = own_lanes()
    mean, slope, level, tilt = (scales_ref[row : row + 1, lanes] for row in range(4))
    return total_ref[:, lanes] * slope - level - (value_ref[:, lanes] - mean) * tilt


def turn_kernel(
    grad_ref, mask_ref, weights_ref, middle_ref, table_ref, total_ref, sums_ref, taps_ref, *, cols
):
    begin_back(grad_ref, weights_ref.at[1], mask_ref, taps_ref, total_ref, cols)
    sums_ref[0:8, :], sums_ref[8:16, :] = finish_back(
        weights_ref.at[1],
        mask_ref,
        taps_ref,
        total_ref,
        lambda rows: middle_ref[rows, :],
        table_ref,
        1,
        cols,
    )


def norm_rows(table_ref, which):
    picks = (2 * which, 2 * which + 1, 6 + which, 9 + which)
    return tuple(table_ref[pick : pick + 1, :] for pick in picks)


def build_masks(ids_ref, mask_ref, lanes_ref, id_rows_ref, id_cols_ref, cols):
    rows = ids_ref.shape[1]

    def one_row(row, carry):
        here = ids_ref[0, row]
        place = pl.ds(pl.multiple_of(row * cols, cols), cols)
        id_rows_ref[place, :] = jnp.full((cols, LANES), here, jnp.int32)
        for side, other in ((0, row - 1), (1, row + 1)):
            inside = jnp.logical_and(other >= 0, other < rows)
            other_id = ids_ref[0, jnp.clip(other, 0, rows - 1)]
            same = jnp.where(jnp.logical_and(inside, other_id == here), 1.0, 0.0)
            mask_ref[side, place, :] = jnp.full((cols, LANES), same, jnp.float32)
        return carry

    lax.fori_loop(0, rows, one_row, 0)
    lane = lax.broadcasted_iota(jnp.int32, (8, LANES), 1)
    each = LANES // cols
    for block in range(rows // each):
        ids = jnp.full((8, LANES), ids_ref[0, block * each], jnp.int32)
        for step in range(1, each):
            ids = jnp.where(lane >= step * cols, ids_ref[0, block * each + step], ids)
        id_cols_ref[:, block * LANES : (block + 1) * LANES] = ids
    ids = id_cols_ref[...].astype(jnp.float32)
    pixels = ids.shape[1]
    pixel = lax.broadcasted_iota(jnp.int32, ids.shape, 1)
    above = jnp.where(pixel < cols, -1.0, pltpu.roll(ids, cols, 1))
    below = jnp.where(pixel >= pixels - cols, -1.0, pltpu.roll(ids, pixels - cols, 1))
    lanes_ref[0:1, :] = jnp.where(above == ids, 1.0, 0.0)[0:1]
    lanes_ref[1:2, :] = jnp.where(below == ids, 1.0, 0.0)[0:1]


def place_pieces(pieces, whole_ref, sems):
    own_pixels = whole_ref.shape[0] // len(pieces)
    height = lax.axis_index("height")
    copies = []
    for place, piece in enumerate(pieces):
        start = pl.multiple_of((height ^ place) * own_pixels, own_pixels)
        rows = pl.ds(start, own_pixels)
        copies.append(pltpu.make_async_copy(piece, whole_ref.at[rows, :], sems.at[place]))
    return copies


def hold_kernel(
    ids_hbm,
    gains_hbm,
    shifts_hbm,
    biases_hbm,
    weights_hbm,
    qkv_hbm,
    proj_hbm,
    qv_bias_hbm,
    proj_bias_hbm,
    weights_ref,
    turned_ref,
    qkv_ref,
    proj_ref,
    table_ref,
    mask_ref,
    lanes_ref,
    id_rows_ref,
    id_cols_ref,
    ids_ref,
    gains_ref,
    shifts_ref,
    biases_ref,
    qv_bias_ref,
    proj_bias_ref,
    sems,
    *,
    cols,
):
    channels = weights_ref.shape[-1]
    small = [
        (ids_hbm, ids_ref),
        (gains_hbm, gains_ref),
        (shifts_hbm, shifts_ref),
        (biases_hbm, biases_ref),
        (qv_bias_hbm, qv_bias_ref),
        (proj_bias_hbm, proj_bias_ref),
    ]
    large = [(weights_hbm, weights_ref), (qkv_hbm, qkv_ref), (proj_hbm, proj_ref)]
    for which in range(2):
        for row_tap in range(3):
            for col_tap in range(3):
                place = slice(col_tap * channels, (col_tap + 1) * channels)
                large.append(
                    (
                        weights_hbm.at[which, 2 - row_tap, 2 - col_tap],
                        turned_ref.at[which, row_tap, :, place],
                    )
                )
    copies = [
        pltpu.make_async_copy(source, target, sems.at[index])
        for index, (source, target) in enumerate(small + large)
    ]
    for copy in copies:
        copy.start()
    for copy in copies[: len(small)]:
        copy.wait()
    build_masks(ids_ref, mask_ref, lanes_ref, id_rows_ref, id_cols_ref, cols)
    table_ref[6:9, :] = gains_ref[...]
    table_ref[9:12, :] = shifts_ref[...]
    table_ref[12:14, :] = biases_ref[...]
    table_ref[14:16, :] = qv_bias_ref[...]
    table_ref[16:17, :] = proj_bias_ref[...]
    for copy in copies[len(small) :]:
        copy.wait()


def conv_kernel(*refs, cols, count):
    pieces, refs = refs[:count], refs[count:]
    (
        weights_ref,
        params_ref,
        mask_ref,
        features_ref,
        act_one_ref,
        middle_ref,
        act_two_ref,
        residual_ref,
        table_ref,
        own_ref,
        taps_ref,
        sem,
    ) = refs
    pixels, channels = features_ref.shape
    wide = jnp.float32
    own_copy = pltpu.make_async_copy(pieces[0], own_ref, sem)
    own_copy.start()
    table_ref[...] = params_ref[...]
    clear_edges(taps_ref, cols)

    def read_input(rows):
        return features_ref[rows, :].astype(wide)

    def read_middle(rows):
        return middle_ref[rows, :]

    height = lax.axis_index("height")
    own_pixels = pixels // count
    seen = RunningStats(channels)
    for place in list(range(1, count)) + [0]:
        if place == 0:
            own_copy.wait()
        piece = (pieces[place] if place else own_ref)[...]
        start = pl.multiple_of((height ^ place) * own_pixels, own_pixels)
        features_ref[pl.ds(start, own_pixels), :] = piece
        seen.add(piece.astype(wide))
    table_ref[0:1, :], table_ref[1:2, :] = seen.finish(pixels)
    seen = RunningStats(channels)

    def keep(rows, value):
        seen.add(value)
        return value

    run_conv(
        taps_ref,
        product_forward(weights_ref.at[0]),
        mask_ref,
        middle_ref,
        activation(read_input, *norm_rows(table_ref, 0), act_one_ref, taps_ref, cols),
        lambda rows, part: part + table_ref[12:13, :],
        keep,
        cols,
    )
    table_ref[2:3, :], table_ref[3:4, :] = seen.finish(pixels)
    seen = RunningStats(channels)
    run_conv(
        taps_ref,
        product_forward(weights_ref.at[1]),
        mask_ref,
        residual_ref,
        activation(read_middle, *norm_rows(table_ref, 1), act_two_ref, taps_ref, cols),
        lambda rows, part: part + (read_input(rows) + table_ref[13:14, :]),
        keep,
        cols,
    )
    table_ref[4:5, :], table_ref[5:6, :] = seen.finish(pixels)


def score_kernel(
    qkv_ref,
    proj_ref,
    residual_ref,
    table_ref,
    id_rows_ref,
    id_cols_ref,
    normed_ref,
    query_ref,
    key_ref,
    value_ref,
    soft_ref,
    out_flip_ref,
    output_ref,
    value_flip_ref,
    *scores_refs,
    score_scale,
):
    pixels, channels = residual_ref.shape
    own_pixels = output_ref.shape[0]
    wide = jnp.float32
    exponent = score_scale * 1.4426950408889634
    mean, inverse, gain, shift = norm_rows(table_ref, 2)
    scale = inverse * gain

    def normalise(start):
        rows = slice(start, start + KEY_ROWS)
        normed = (residual_ref[rows, :] - mean) * scale + shift
        normed_ref[rows, :] = normed.astype(jnp.bfloat16)

    def project(start):
        rows = slice(start, start + KEY_ROWS)
        normed = normed_ref[rows, :]
        query_ref[rows, :] = (
            jnp.dot(normed, qkv_ref[:, 0:channels], preferred_element_type=wide)
            + table_ref[14:15, :]
        ).astype(jnp.bfloat16)
        key_ref[rows, :] = jnp.dot(
            normed, qkv_ref[:, channels : 2 * channels], preferred_element_type=wide
        ).astype(jnp.bfloat16)
        values = (
            jnp.dot(normed, qkv_ref[:, 2 * channels :], preferred_element_type=wide)
            + table_ref[15:16, :]
        ).astype(jnp.bfloat16)
        value_ref[rows, :] = values
        value_flip_ref[:, rows] = values.T

    normalise(0)
    for start in range(0, pixels, KEY_ROWS):
        if start + KEY_ROWS < pixels:
            normalise(start + KEY_ROWS)
        project(start)
    block = scores_refs[0].shape[1]
    steps = range(0, pixels, KEY_ROWS)

    def score(index):
        rows = slice(index * block, (index + 1) * block)
        for start in steps:
            keys = slice(start, start + KEY_ROWS)
            scores = lax.dot_general(
                key_ref[keys, :],
                query_ref[rows, :],
                (((1,), (1,)), ((), ())),
                preferred_element_type=wide,
            )
            same = widen(id_rows_ref[keys, :], block) == id_cols_ref[0:1, rows]
            scores_refs[index][keys, :] = jnp.where(same, scores, masked_score)

    def soften(index):
        rows = slice(index * block, (index + 1) * block)
        scores_ref = scores_refs[index]
        peak = jnp.full((8, block), masked_score, wide)
        for start in steps:
            scores = scores_ref[start : start + KEY_ROWS, :]
            peak = jnp.maximum(peak, jnp.max(scores.reshape(-1, 8, block), axis=0))
        peak = jnp.max(peak, axis=0, keepdims=True)
        total = jnp.zeros((8, block), wide)
        for start in steps:
            keys = slice(start, start + KEY_ROWS)
            powers = jnp.exp2((scores_ref[keys, :] - peak) * exponent)
            scores_ref[keys, :] = powers
            total = total + fold(powers)
        share = 1.0 / column_total(total)
        for start in steps:
            keys = slice(start, start + KEY_ROWS)
            soft_ref[keys, rows] = (scores_ref[keys, :] * share).astype(jnp.bfloat16)

    score(0)
    for index in range(len(scores_refs)):
        if index + 1 < len(scores_refs):
            score(index + 1)
        soften(index)

    def collect(rows, carry):
        out_flip_ref[rows, :] = jnp.dot(
            value_flip_ref[rows, :], soft_ref[...], preferred_element_type=wide
        ).astype(jnp.bfloat16)
        return carry

    each_block(channels, channels // 2, collect)
    height = lax.axis_index("height")
    own = pl.ds(pl.multiple_of(height * own_pixels, own_pixels), own_pixels)
    output_ref[...] = (
        residual_ref[own, :]
        + lax.dot_general(
            out_flip_ref[:, own],
            proj_ref[...],
            (((0,), (0,)), ((), ())),
            preferred_element_type=wide,
        )
        + table_ref[16:17, :]
    ).astype(jnp.bfloat16)


def own_quarter():
    height = lax.axis_index("height")
    return (height & 1) * 2 + ((height >> 1) & 1)


def send_order(source_ref, targets, axis, share):
    me = lax.axis_index("canvas")
    for step, target in enumerate(targets):
        place = pl.ds(pl.multiple_of((me ^ step) * share, share), share)
        target[...] = source_ref[place, :] if axis == 0 else source_ref[:, place]


def attention_kernel(
    proj_ref,
    normed_ref,
    query_ref,
    key_ref,
    value_ref,
    soft_ref,
    out_flip_ref,
    *refs,
    score_scale,
    count,
):
    pieces, (grad_ref, packed_ref, sums_ref), refs = (
        refs[:count],
        refs[count : count + 3],
        refs[count + 3 :],
    )
    pixels, channels = normed_ref.shape
    blocks = pixels // SCORE_ROWS
    grads_refs, refs = refs[-blocks:], refs[:-blocks]
    *mixed_refs, mixed_ref, key_flip_ref, back_ref, score_grad_ref, flip_ref, sems = refs
    wide = jnp.float32
    copies = place_pieces(pieces, grad_ref, sems)
    for copy in copies:
        copy.start()
    quarter = channels // 4
    own = pl.ds(pl.multiple_of(own_quarter() * quarter, quarter), quarter)
    flip_ref[...] = normed_ref[:, own].T
    key_flip_ref[...] = key_ref[...].T
    for copy in copies:
        copy.wait()
    block, count = SCORE_ROWS, blocks
    steps = range(0, pixels, KEY_ROWS)

    def block_rows(index):
        return slice(index * block, (index + 1) * block)

    for index in range(count):
        back_ref[block_rows(index), :] = lax.dot_general(
            grad_ref[block_rows(index), :],
            proj_ref[...],
            (((1,), (1,)), ((), ())),
            preferred_element_type=wide,
        ).astype(jnp.bfloat16)

    def weigh(index):
        total = jnp.zeros((8, block), wide)
        for start in steps:
            keys = slice(start, start + KEY_ROWS)
            weight_grad = lax.dot_general(
                value_ref[keys, :],
                back_ref[block_rows(index), :],
                (((1,), (1,)), ((), ())),
                preferred_element_type=wide,
            )
            grads_refs[index][keys, :] = weight_grad
            total = total + fold(soft_ref[keys, block_rows(index)].astype(wide) * weight_grad)
        return column_total(total)

    def slope(index, dots):
        for start in steps:
            keys = slice(start, start + KEY_ROWS)
            weights = soft_ref[keys, block_rows(index)].astype(wide)
            score_grad_ref[keys, block_rows(index)] = (
                weights * (grads_refs[index][keys, :] - dots)
            ).astype(jnp.bfloat16)

    dots = weigh(0)
    for index in range(count):
        now, rows = dots, block_rows(index)
        if index + 1 < count:
            dots = weigh(index + 1)
        slope(index, now)
        packed_ref[rows, 2 * channels :] = jnp.dot(
            soft_ref[rows, :], back_ref[...], preferred_element_type=wide
        ).astype(jnp.bfloat16)
        query_grad = jnp.dot(
            key_flip_ref[...], score_grad_ref[:, rows], preferred_element_type=wide
        )
        packed_ref[rows, 0:channels] = (query_grad * score_scale).astype(jnp.bfloat16).T
    for index in range(count):
        rows = block_rows(index)
        packed_ref[rows, channels : 2 * channels] = (
            jnp.dot(score_grad_ref[rows, :], query_ref[...], preferred_element_type=wide)
            * score_scale
        ).astype(jnp.bfloat16)

    def pack(rows, carry):
        return (
            carry[0] + fold(packed_ref[rows, 0:channels].astype(wide)),
            carry[1] + fold(packed_ref[rows, 2 * channels :].astype(wide)),
            carry[2] + fold(grad_ref[rows, :].astype(wide)),
        )

    zeros = jnp.zeros((8, channels), wide)
    totals = zeros, zeros, zeros
    for start in range(0, pixels, CHUNK):
        totals = pack(pl.ds(start, CHUNK), totals)
    sums_ref[...] = jnp.zeros(sums_ref.shape, wide)
    for row, total in enumerate(totals):
        sums_ref[8 + row : 9 + row, :] = column_total(total)
    mixed_ref[:, 0 : 3 * channels] = jnp.dot(
        flip_ref[...], packed_ref[...], preferred_element_type=wide
    ).astype(jnp.bfloat16)
    mixed_ref[:, 3 * channels :] = jnp.dot(
        out_flip_ref[own, :], grad_ref[...], preferred_element_type=wide
    ).astype(jnp.bfloat16)
    send_order(mixed_ref, mixed_refs, 0, quarter // len(mixed_refs))


def third_kernel(
    qkv_ref,
    grad_ref,
    packed_ref,
    residual_ref,
    table_ref,
    act_two_ref,
    lanes_ref,
    old_sums_ref,
    residual_grad_ref,
    grad_two_ref,
    sums_ref,
    keep_ref,
    send_ref,
    total_ref,
    flip_ref,
    columns_ref,
    part_ref,
    *,
    cols,
):
    pixels, channels = residual_ref.shape
    block = FILL_ROWS
    wide = jnp.float32
    mean, inverse, gain, shift = norm_rows(table_ref, 2)
    zeros = jnp.zeros((8, channels), wide)

    sums = (zeros, zeros)
    for start in range(0, pixels, block):
        rows = pl.ds(start, block)
        normed_grad = lax.dot_general(
            packed_ref[rows, :], qkv_ref[...], (((1,), (1,)), ((), ())), preferred_element_type=wide
        )
        total_ref[rows, :] = normed_grad
        centered = residual_ref[rows, :] - mean
        sums = sums[0] + fold(normed_grad), sums[1] + fold(normed_grad * centered)
    sums = sums[0], sums[1] * inverse
    sums_ref[...] = old_sums_ref[...]
    sums_ref[5:6, :] = column_total(sums[1])
    sums_ref[6:7, :] = column_total(sums[0])
    back = norm_back(
        total_ref, False, sums, lambda rows: residual_ref[rows, :], table_ref, 2, pixels
    )

    def finish(rows, carry):
        total = grad_ref[rows, :].astype(wide) + back(rows, rows)
        residual_grad_ref[rows, :] = total
        low = total.astype(jnp.bfloat16)
        grad_two_ref[rows, :] = low
        return carry + fold(low.astype(wide))

    sums_ref[7:8, :] = column_total(each_chunk(pixels, finish, zeros))
    narrow = grad_two_ref[:, own_lanes()]
    weight_part(act_two_ref, narrow, lanes_ref, flip_ref, columns_ref, part_ref, cols)
    keep_half(part_ref, 2, 1, keep_ref, send_ref)


def second_kernel(
    total_ref,
    partial_ref,
    middle_ref,
    table_ref,
    act_one_ref,
    lanes_ref,
    old_sums_ref,
    grad_one_ref,
    sums_ref,
    keep_ref,
    send_ref,
    flip_ref,
    columns_ref,
    part_ref,
    scales_ref,
    *,
    cols,
):
    pixels, channels = middle_ref.shape
    sums = partial_ref[0:8, :], partial_ref[8:16, :]
    back = norm_back(
        total_ref, True, sums, lambda rows: middle_ref[rows, :], table_ref, 1, pixels, scales_ref
    )
    narrow = narrow_back(total_ref, middle_ref, scales_ref).astype(jnp.bfloat16)
    weight_part(act_one_ref, narrow, lanes_ref, flip_ref, columns_ref, part_ref, cols)
    sums_ref[...] = old_sums_ref[...]
    sums_ref[2:3, :] = column_total(sums[1])
    sums_ref[3:4, :] = column_total(sums[0])

    def finish(rows, carry):
        low = back(rows, rows).astype(jnp.bfloat16)
        grad_one_ref[rows, :] = low
        return carry + fold(low.astype(jnp.float32))

    zeros = jnp.zeros((8, channels), jnp.float32)
    total = zeros
    for start in range(0, pixels, CHUNK):
        total = finish(pl.ds(start, CHUNK), total)
    sums_ref[4:5, :] = column_total(total)
    keep_half(part_ref, 1, 2, keep_ref, send_ref)


def keep_half(part_ref, near, far, keep_ref, send_ref):
    me = lax.axis_index("canvas")
    rows, width = part_ref.shape[0], keep_ref.shape[1]
    for target_ref, flip in ((keep_ref, 0), (send_ref, near)):
        for slot in range(2):
            owner = me ^ flip ^ (slot * far)
            place = pl.ds(pl.multiple_of(owner * width, width), width)
            target_ref[slot * rows : (slot + 1) * rows, :] = part_ref[:, place]


def first_kernel(
    grad_one_ref,
    features_ref,
    table_ref,
    mask_ref,
    old_sums_ref,
    weights_ref,
    own_ref,
    sums_ref,
    partial_ref,
    total_ref,
    taps_ref,
    *,
    cols,
):
    def read(rows):
        return features_ref[rows, :].astype(jnp.float32)

    weights = weights_ref.at[0]
    begin_back(grad_one_ref, weights, mask_ref, taps_ref, total_ref, cols)
    sums = finish_back(weights, mask_ref, taps_ref, total_ref, read, table_ref, 0, cols)
    partial_ref[0:8, :], partial_ref[8:16, :] = sums
    sums_ref[...] = old_sums_ref[...]
    sums_ref[0:1, :] = column_total(sums[1])
    sums_ref[1:2, :] = column_total(sums[0])
    count = own_ref.shape[0]
    own = pl.ds(pl.multiple_of(lax.axis_index("height") * count, count), count)
    own_ref[...] = total_ref[own, :]


def own_kernel(
    own_ref, partial_ref, features_ref, residual_grad_ref, table_ref, input_grad_ref
):
    def read(rows):
        return features_ref[rows, :].astype(jnp.float32)

    sums = partial_ref[0:8, :], partial_ref[8:16, :]
    pixels = features_ref.shape[0]
    back = norm_back(own_ref, True, sums, read, table_ref, 0, pixels)
    count = own_ref.shape[0]
    own = pl.ds(pl.multiple_of(lax.axis_index("height") * count, count), count)
    total = residual_grad_ref[own, :] + back(own, slice(0, count))
    input_grad_ref[...] = total.astype(jnp.bfloat16)


def place_kernel(*refs):
    joints, packed_ref = refs[:-1], refs[-1]
    share = packed_ref.shape[0] // len(joints)
    me = lax.axis_index("canvas")
    for step, joint in enumerate(joints):
        place = pl.ds(pl.multiple_of((me ^ step) * share, share), share)
        packed_ref[place, :] = joint[...]


def spread_quarters(packed, flips, qkv_ref, proj_ref, qkv_hbm, proj_hbm, sems):
    quarter = packed[0].shape[0]
    inner = qkv_ref.shape[2]
    copies = []
    for index, packed_ref in enumerate(packed):
        owner = own_quarter() ^ flips[index]
        rows = pl.ds(pl.multiple_of(owner * quarter, quarter), quarter)
        qkv_ref[index] = packed_ref[:, 0:inner].astype(jnp.float32)
        proj_ref[index] = packed_ref[:, inner:].astype(jnp.float32)
        for which, (held, target) in enumerate(((qkv_ref, qkv_hbm), (proj_ref, proj_hbm))):
            copy = pltpu.make_async_copy(held.at[index], target.at[rows, :], sems.at[index, which])
            copy.start()
            copies.append(copy)
    return copies


def join_kernel(*refs):
    packed, (qkv_hbm, proj_hbm, qkv_ref, proj_ref, sems) = refs[:-5], refs[-5:]
    copies = spread_quarters(
        packed, range(len(packed)), qkv_ref, proj_ref, qkv_hbm, proj_hbm, sems
    )
    for copy in copies:
        copy.wait()


def halve_kernel(keep_ref, got_ref, hold_ref, send_ref):
    total = keep_ref[...].astype(jnp.float32) + got_ref[...].astype(jnp.float32)
    rows = hold_ref.shape[0]
    hold_ref[...] = total[0:rows]
    send_ref[0:rows, :] = total[rows:].astype(jnp.bfloat16)


def halve_sums_kernel(
    keep_one_ref,
    got_one_ref,
    keep_two_ref,
    got_two_ref,
    sums_ref,
    hold_ref,
    send_ref,
    hold_two_ref,
    send_two_ref,
):
    halve_kernel(keep_one_ref, got_one_ref, hold_ref, send_ref)
    halve_kernel(keep_two_ref, got_two_ref, hold_two_ref, send_two_ref)
    rows = hold_ref.shape[0]
    low = sums_ref[...].astype(jnp.bfloat16)
    count, width = low.shape
    for block in range(width // LANES):
        place = slice(rows + block * count, rows + (block + 1) * count)
        piece = low[:, block * LANES : (block + 1) * LANES]
        send_ref[place, :] = piece
        send_two_ref[place, :] = piece


def unpack_sums(got_ref, rows, count, width):
    blocks = [
        got_ref[start : start + count, :].astype(jnp.float32)
        for start in range(rows, rows + width // LANES * count, count)
    ]
    return jnp.concatenate(blocks, axis=1)


def sums_kernel(
    sums_ref,
    far_ref,
    hold_one_ref,
    got_one_ref,
    hold_two_ref,
    got_two_ref,
    share_ref,
    gains_ref,
    shifts_ref,
    conv_ref,
    qv_ref,
    bias_ref,
):
    rows = hold_one_ref.shape[0]
    for which, (hold_ref, got_ref) in enumerate(
        ((hold_one_ref, got_one_ref), (hold_two_ref, got_two_ref))
    ):
        total = hold_ref[...] + got_ref[0:rows, :].astype(jnp.float32)
        share_ref[which] = total.reshape(share_ref.shape[1:])
    total = sums_ref[...] + far_ref[...]
    for got_ref in (got_one_ref, got_two_ref):
        total = total + unpack_sums(got_ref, rows, *total.shape)
    for row, start in enumerate((0, 2, 5)):
        gains_ref[row : row + 1, :] = total[start : start + 1]
        shifts_ref[row : row + 1, :] = total[start + 1 : start + 2]
    conv_ref[0:1, :] = total[4:5]
    conv_ref[1:2, :] = total[7:8]
    qv_ref[...] = total[8:10]
    bias_ref[...] = total[10:11]


def call_kernel(kernel, outputs, scratch, operands, places, flops, limit, out_places=None, aliases={}):
    out_places = out_places or "v" * len(outputs)
    spaces = {
        "v": pl.BlockSpec(memory_space=pltpu.VMEM),
        "s": pl.BlockSpec(memory_space=pltpu.SMEM),
        "h": pl.BlockSpec(memory_space=pl.ANY),
        "o": pl.BlockSpec(memory_space=pltpu.VMEM),
        "a": pl.BlockSpec(memory_space=pl.ANY),
    }
    moved = 8 * flops // LANES
    held = {"v": pltpu.VMEM, "h": pltpu.HBM, "o": jax.ShapeDtypeStruct}
    operands = [
        pltpu.with_memory_space_constraint(array, pltpu.HBM) if place == "h" else array
        for array, place in zip(operands, places)
    ]
    return pl.pallas_call(
        kernel,
        out_shape=[held[place](*output) for output, place in zip(outputs, out_places)],
        in_specs=[spaces[place] for place in places],
        out_specs=[spaces[place] for place in out_places],
        scratch_shapes=scratch,
        input_output_aliases=aliases,
        compiler_params=pltpu.CompilerParams(vmem_limit_bytes=limit * 2**20),
        cost_estimate=pl.CostEstimate(flops=flops, bytes_accessed=moved, transcendentals=0),
    )(*operands)


def send_height(block, step):
    size = lax.axis_size("height")
    return lax.ppermute(block, "height", [(i, i ^ step) for i in range(size)])


def with_cores(blocks):
    return [piece for block in blocks for piece in (block, send_height(block, 1))]


def send_canvas(block, step):
    size = lax.axis_size("canvas")
    return lax.ppermute(block, "canvas", [(i, i ^ step) for i in range(size)])


def trade_canvas(pieces):
    return [pieces[0]] + [send_canvas(piece, step) for step, piece in enumerate(pieces) if step]


def whole_canvas(
    features,
    tile_ids,
    norm_gains,
    norm_shifts,
    conv_weights,
    conv_biases,
    qkv_weight,
    qv_bias,
    proj_weight,
    proj_bias,
    cotangent,
):
    height_size = lax.axis_size("height")
    canvas_size = lax.axis_size("canvas")
    local_rows, cols, channels = features.shape[1:]
    all_rows = tile_ids.shape[1]
    pixels = all_rows * cols
    own_pixels = local_rows * cols
    out_share = channels // height_size
    ci_share = channels // canvas_size
    quarter = channels // 4
    row_share = quarter // canvas_size
    low, wide = jnp.bfloat16, jnp.float32

    own_features = features.reshape(own_pixels, channels)
    own_grad = cotangent.reshape(own_pixels, channels)
    steps = range(2, height_size, 2)
    held_features = [own_features] + [send_height(own_features, step) for step in steps]
    plane = ((pixels, channels), low)
    plane_wide = ((pixels, channels), wide)
    sums_shape = ((16, channels), wide)
    mixed_shapes = [((row_share, 4 * channels), low)] * canvas_size
    taps = pltpu.VMEM((pixels + 2 * cols, 3 * channels), low)
    held_wide = pltpu.VMEM((pixels, channels), wide)
    flipped = pltpu.VMEM((channels, pixels), low)
    narrow = pltpu.VMEM((NARROW, pixels), low)
    columns = pltpu.VMEM((9 * out_share, pixels), low)
    part_held = pltpu.VMEM((9 * out_share, channels), low)
    sem = pltpu.SemaphoreType.DMA
    conv_flops = 2 * 9 * pixels * channels * channels
    dot_flops = 2 * pixels * channels * channels
    score_flops = 2 * pixels * pixels * channels
    scale = channels ** (-0.5)

    (
        held_conv,
        turned,
        held_qkv,
        held_proj,
        params,
        mask,
        lane_mask,
        id_rows,
        id_cols,
    ) = call_kernel(
        functools.partial(hold_kernel, cols=cols),
        [
            (conv_weights.shape, low),
            ((2, 3, channels, 3 * channels), low),
            (qkv_weight.shape, low),
            (proj_weight.shape, low),
            ((24, channels), wide),
            ((2, pixels, LANES), wide),
            ((8, pixels), wide),
            ((pixels, LANES), jnp.int32),
            ((8, pixels), jnp.int32),
        ],
        [
            pltpu.SMEM(tile_ids.shape, jnp.int32),
            pltpu.VMEM(norm_gains.shape, wide),
            pltpu.VMEM(norm_shifts.shape, wide),
            pltpu.VMEM(conv_biases.shape, wide),
            pltpu.VMEM(qv_bias.shape, wide),
            pltpu.VMEM((1, channels), wide),
            sem((27,)),
        ],
        [
            tile_ids,
            norm_gains,
            norm_shifts,
            conv_biases,
            conv_weights,
            qkv_weight,
            proj_weight,
            qv_bias,
            proj_bias.reshape(1, channels),
        ],
        "h" * 9,
        conv_flops,
        8,
    )
    held_features[1:] = [
        lax.optimization_barrier((params, block))[1] for block in held_features[1:]
    ]
    pieces = with_cores(held_features)
    far_grad, *pieces[4::2] = lax.optimization_barrier((own_grad, *held_features[2:]))
    held_grads = [own_grad, send_height(own_grad, 2)]
    held_grads[1], pieces[2] = lax.optimization_barrier((held_grads[1], held_features[1]))
    held_grads += [send_height(far_grad, step) for step in steps[1:]]

    all_features, act_one, middle, act_two, residual, table = call_kernel(
        functools.partial(conv_kernel, cols=cols, count=height_size),
        [plane, plane, plane_wide, plane, plane_wide, ((24, channels), wide)],
        [pltpu.VMEM((own_pixels, channels), low), taps, sem],
        [*pieces, held_conv, params, mask],
        "h" + "v" * (height_size + 2),
        2 * conv_flops,
        16,
    )
    residual, *held_grads = lax.optimization_barrier((residual, *held_grads))
    grad_pieces = with_cores(held_grads)
    normed, query, key, value, soft, out_flip, output = call_kernel(
        functools.partial(score_kernel, score_scale=scale),
        [
            plane,
            plane,
            plane,
            plane,
            ((pixels, pixels), low),
            ((channels, pixels), low),
            ((own_pixels, channels), low),
        ],
        [
            flipped,
            *[pltpu.VMEM((pixels, SCORE_ROWS), wide)] * (pixels // SCORE_ROWS),
        ],
        [
            held_qkv,
            held_proj,
            residual,
            table,
            id_rows,
            id_cols,
        ],
        "vvvvvv",
        3 * dot_flops + 2 * score_flops,
        20,
        "v" * 6 + "o",
    )
    normed, *grad_pieces = lax.optimization_barrier((normed, *grad_pieces))
    all_grad, packed, sums, *mixed = call_kernel(
        functools.partial(attention_kernel, score_scale=scale, count=height_size),
        [plane, ((pixels, 3 * channels), low), sums_shape, *mixed_shapes],
        [
            pltpu.VMEM((quarter, 4 * channels), low),
            flipped,
            pltpu.VMEM((pixels, channels), low),
            pltpu.VMEM((pixels, pixels), low),
            pltpu.VMEM((quarter, pixels), low),
            sem((height_size,)),
            *[pltpu.VMEM((pixels, SCORE_ROWS), wide)] * (pixels // SCORE_ROWS),
        ],
        [held_proj, normed, query, key, value, soft, out_flip, *grad_pieces],
        "vvvvvvvh" + "a" * (height_size - 1),
        3 * dot_flops + 4 * score_flops,
        20,
    )
    mixed = trade_canvas(mixed)
    halves = [((18 * out_share, ci_share), low)] * 2
    residual_grad, grad_two, sums, keep_two, send_two = call_kernel(
        functools.partial(third_kernel, cols=cols),
        [plane_wide, plane, sums_shape, *halves],
        [held_wide, narrow, columns, part_held],
        [held_qkv, all_grad, packed, residual, table, act_two, lane_mask, sums],
        "vvvvvvvv",
        3 * dot_flops + conv_flops // height_size,
        16,
    )
    grad_two, *mixed = lax.optimization_barrier((grad_two, *mixed))
    mixed_sum = mixed[0].astype(wide)
    for piece in mixed[1:]:
        mixed_sum = mixed_sum + piece.astype(wide)
    joints = trade_canvas([mixed_sum.astype(low)] * canvas_size)
    act_two_grad, partial_sums = call_kernel(
        functools.partial(turn_kernel, cols=cols),
        [plane_wide, sums_shape],
        [taps],
        [grad_two, mask, turned, middle, table],
        "vvvvv",
        conv_flops,
        16,
    )
    act_two_grad, *joints = lax.optimization_barrier((act_two_grad, *joints))
    (own_mixed,) = call_kernel(
        place_kernel,
        [((quarter, 4 * channels), low)],
        [],
        joints,
        "v" * canvas_size,
        1,
        12,
    )
    own_mixed, send_two = lax.optimization_barrier((own_mixed, send_two))
    got_two = send_canvas(send_two, 2)
    chip_mixed = send_height(own_mixed, 2)
    core_mixed = send_height(own_mixed, 1)
    grad_one, sums, keep_one, send_one = call_kernel(
        functools.partial(second_kernel, cols=cols),
        [plane, sums_shape, *halves],
        [narrow, columns, part_held, pltpu.VMEM((8, channels), wide)],
        [act_two_grad, partial_sums, middle, table, act_one, lane_mask, sums],
        "vvvvvvv",
        1,
        16,
    )
    got_one = send_canvas(send_one, 1)

    own_total, sums, partial_sums = call_kernel(
        functools.partial(first_kernel, cols=cols),
        [((own_pixels, channels), wide), sums_shape, sums_shape],
        [held_wide, taps],
        [grad_one, all_features, table, mask, sums, turned],
        "vvvvvv",
        1,
        20,
    )
    (input_grad,) = call_kernel(
        own_kernel,
        [((own_pixels, channels), low)],
        [],
        [own_total, partial_sums, all_features, residual_grad, table],
        "vvvvv",
        dot_flops // 4,
        12,
        "o",
    )
    input_grad, sums, core_mixed, got_one, got_two = lax.optimization_barrier(
        (input_grad, sums, core_mixed, got_one, got_two)
    )
    share_rows = 9 * out_share
    send_rows = share_rows + sums_shape[0][0] * channels // LANES
    hold_one, send_one, hold_two, send_two = call_kernel(
        halve_sums_kernel,
        [((share_rows, ci_share), wide), ((send_rows, ci_share), low)] * 2,
        [],
        [keep_one, got_one, keep_two, got_two, sums],
        "vvvvv",
        1,
        12,
    )
    got_two = send_canvas(send_two, 1)
    got_one = send_canvas(send_one, 2)
    far_sums = send_canvas(sums, 3)
    chip_mixed, hold_one = lax.optimization_barrier((chip_mixed, hold_one))
    both_mixed = send_height(chip_mixed, 1)
    qkv_grad, proj_grad = call_kernel(
        join_kernel,
        [(qkv_weight.shape, wide), (proj_weight.shape, wide)],
        [
            pltpu.VMEM((4, quarter, 3 * channels), wide),
            pltpu.VMEM((4, quarter, channels), wide),
            sem((4, 2)),
        ],
        [own_mixed, chip_mixed, core_mixed, both_mixed],
        "vvvv",
        dot_flops // 4,
        12,
        "hh",
    )
    qkv_grad, got_one, got_two, far_sums = lax.optimization_barrier(
        (qkv_grad, got_one, got_two, far_sums)
    )
    vector_shapes = [norm_gains.shape, norm_shifts.shape, conv_biases.shape, qv_bias.shape]
    conv_grad, gains_grad, shifts_grad, biases_grad, qv_grad, proj_bias_grad = call_kernel(
        sums_kernel,
        [((2, 3, 3, out_share, ci_share), wide)]
        + [(shape, wide) for shape in vector_shapes + [(1, channels)]],
        [],
        [sums, far_sums, hold_one, got_one, hold_two, got_two],
        "vvvvvv",
        1,
        12,
        "o" * 6,
    )
    own_shape = (1, local_rows, cols, channels)
    return (
        output.reshape(own_shape),
        input_grad.reshape(own_shape),
        gains_grad,
        shifts_grad,
        jnp.swapaxes(conv_grad, 3, 4),
        biases_grad,
        qkv_grad,
        qv_grad,
        proj_grad,
        proj_bias_grad.reshape(channels),
    )


def on_device(*arrays):
    features, tile_ids = arrays[0], arrays[1]
    local_rows, cols, channels = features.shape[1:]
    pixels = tile_ids.shape[1] * cols
    height_size, canvas_size = lax.axis_size("height"), lax.axis_size("canvas")
    powers = all(size & (size - 1) == 0 for size in (height_size, canvas_size, cols))
    fits = (
        powers
        and height_size > 2
        and canvas_size == 4
        and channels == LANES * canvas_size
        and pixels <= MOST_PIXELS
        and pixels % FILL_ROWS == 0
        and FILL_ROWS % CHUNK == 0
        and pixels % SCORE_ROWS == 0
        and pixels % KEY_ROWS == 0
        and (local_rows * cols) % LANES == 0
        and CHUNK % cols == 0
        and cols % 16 == 0
        and channels % (LANES * canvas_size) == 0
        and 2 * channels == NARROW * height_size
    )
    return whole_canvas(*arrays) if fits else split_canvas(*arrays)


def solution(mesh):
    in_specs = (
        P("canvas", "height", None, None),
        P("canvas", None),
        P(),
        P(),
        P(),
        P(),
        P(),
        P(),
        P(),
        P(),
        P("canvas", "height", None, None),
    )
    out_specs = (
        P("canvas", "height", None, None),
        P("canvas", "height", None, None),
        P(),
        P(),
        P(None, None, None, "canvas", "height"),
        P(),
        P(),
        P(),
        P(),
        P(),
    )
    return jax.shard_map(
        on_device, mesh=mesh, in_specs=in_specs, out_specs=out_specs, check_vma=False
    )
```

```python
import functools

import jax
import jax.numpy as jnp
from jax import lax
from jax.experimental import pallas as pl
from jax.experimental.pallas import tpu as pltpu
from jax.sharding import PartitionSpec as P

GROUPS = 32


epsilon = 1e-06
masked_score = -1e30
MOST_PIXELS = 1024
LANES = 128
NARROW = 128
CHUNK = 128
FILL_ROWS = 256
QUERY_ROWS = 512
SCORE_ROWS = 256
KEY_ROWS = 256


def extended(block, sides, width):
    for axis, dim in sides:
        count = lax.axis_size(axis)
        forward = [(i, i + 1) for i in range(count - 1)]
        backward = [(target, source) for source, target in forward]
        low = lax.ppermute(
            lax.slice_in_dim(block, block.shape[dim] - width, None, axis=dim), axis, forward
        )
        high = lax.ppermute(lax.slice_in_dim(block, 0, width, axis=dim), axis, backward)
        block = jnp.concatenate([low, block, high], axis=dim)
    return block


def group_total(vector):
    return vector.reshape(GROUPS, -1).sum(axis=1)


def spread_groups(vector, channels):
    return jnp.repeat(vector, channels // GROUPS)


def norm_forward(values, gain, shift, members):
    channels = values.shape[1]
    totals = lax.psum(group_total(jnp.sum(values, axis=0)), "height")
    centered = values - spread_groups(totals / members, channels)
    squares = lax.psum(group_total(jnp.sum(centered * centered, axis=0)), "height")
    inverse = spread_groups(lax.rsqrt(squares / members + epsilon), channels)
    normed = centered * inverse
    return (normed, inverse, normed * gain + shift)


def norm_backward(grad_in, normed, inverse, gain, members):
    channels = grad_in.shape[1]
    scaled = grad_in * gain
    both_sums = lax.psum(
        (group_total(jnp.sum(scaled, axis=0)), group_total(jnp.sum(scaled * normed, axis=0))),
        "height",
    )
    mean_grad = spread_groups(both_sums[0] / members, channels)
    mean_cross = spread_groups(both_sums[1] / members, channels)
    result = inverse * (scaled - mean_grad - normed * mean_cross)
    return (result, jnp.sum(grad_in * normed, axis=0), jnp.sum(grad_in, axis=0))


def swish(values):
    return values * jax.nn.sigmoid(values)


def swish_slope(values):
    sigmoid_part = jax.nn.sigmoid(values)
    return sigmoid_part * (1.0 + values * (1.0 - sigmoid_part))


def tap_columns(padded, row_mask, local_rows, canvas_cols):
    pieces = []
    for row_tap in range(3):
        rows_taken = padded[row_tap : row_tap + local_rows] * row_mask[:, row_tap, None, None]
        for col_tap in range(3):
            pieces.append(rows_taken[:, col_tap : col_tap + canvas_cols])
    stacked = jnp.concatenate(pieces, axis=2)
    return stacked.reshape(local_rows * canvas_cols, stacked.shape[2])


def conv_forward(acts, row_mask, weight, bias):
    local_rows, canvas_cols, channels = acts.shape
    rimmed = extended(acts, (("height", 0),), 1)
    padded = jnp.pad(rimmed, ((0, 0), (1, 1), (0, 0)))
    gathered = tap_columns(padded, row_mask, local_rows, canvas_cols)
    result = (
        jnp.dot(
            gathered, weight.reshape(9 * channels, channels), preferred_element_type=jnp.float32
        )
        + bias
    )
    return (result, gathered)


def conv_backward(grad_low, row_mask, weight, gathered):
    local_rows, canvas_cols, channels = grad_low.shape
    flat_grad = grad_low.reshape(local_rows * canvas_cols, channels)
    weight_grad = lax.dot_general(
        gathered, flat_grad, (((0,), (0,)), ((), ())), preferred_element_type=jnp.float32
    )
    rimmed = extended(grad_low, (("height", 0),), 1)
    padded = jnp.pad(rimmed, ((0, 0), (1, 1), (0, 0)))
    grad_taps = tap_columns(padded, row_mask, local_rows, canvas_cols)
    flipped = jnp.transpose(weight[::-1, ::-1], (0, 1, 3, 2)).reshape(9 * channels, channels)
    input_part = jnp.dot(grad_taps, flipped, preferred_element_type=jnp.float32)
    return (
        input_part,
        weight_grad.reshape(3, 3, channels, channels),
        jnp.sum(flat_grad.astype(jnp.float32), axis=0),
    )


def take_rows(array, offset, count):
    return lax.dynamic_slice_in_dim(array, offset, count)


def score_grads(
    queries, out_grad, log_total, row_dots, query_ids, key_rows, value_rows, key_ids, score_scale
):
    scores = (
        lax.dot_general(
            queries, key_rows, (((1,), (1,)), ((), ())), preferred_element_type=jnp.float32
        )
        * score_scale
    )
    same_tile = query_ids[:, None] == key_ids[None, :]
    softmax_block = jnp.exp(jnp.where(same_tile, scores - log_total[:, None], masked_score))
    weight_grad = lax.dot_general(
        out_grad, value_rows, (((1,), (1,)), ((), ())), preferred_element_type=jnp.float32
    )
    score_grad = (softmax_block * (weight_grad - row_dots[:, None])).astype(jnp.bfloat16)
    return (softmax_block.astype(jnp.bfloat16), score_grad)


def split_canvas(
    features,
    tile_ids,
    norm_gains,
    norm_shifts,
    conv_weights,
    conv_biases,
    qkv_weight,
    qv_bias,
    proj_weight,
    proj_bias,
    cotangent,
):
    height_size = lax.axis_size("height")
    local_rows = features.shape[1]
    canvas_cols = features.shape[2]
    channels = features.shape[3]
    pixels = local_rows * canvas_cols
    row_ids = tile_ids[0]
    all_rows = row_ids.shape[0]
    members = float(all_rows * canvas_cols * (channels // GROUPS))
    score_scale = channels ** (-0.5)
    first_row = lax.axis_index("height") * local_rows
    edge_ids = jnp.full((1,), -1, jnp.int32)
    padded_ids = jnp.concatenate([edge_ids, row_ids, edge_ids])
    near_ids = lax.dynamic_slice_in_dim(padded_ids, first_row, local_rows + 2)
    own_rows = near_ids[1 : local_rows + 1]
    row_mask = jnp.stack(
        [near_ids[row_tap : row_tap + local_rows] == own_rows for row_tap in range(3)], axis=1
    ).astype(jnp.bfloat16)
    key_ids = jnp.repeat(row_ids, canvas_cols)
    query_ids = jnp.repeat(own_rows, canvas_cols)
    grid_shape = (local_rows, canvas_cols, channels)
    inputs = features[0].reshape(pixels, channels).astype(jnp.float32)
    normed_one, inverse_one, pre_one = norm_forward(inputs, norm_gains[0], norm_shifts[0], members)
    act_one = swish(pre_one).astype(jnp.bfloat16).reshape(grid_shape)
    middle, taps_one = conv_forward(act_one, row_mask, conv_weights[0], conv_biases[0])
    normed_two, inverse_two, pre_two = norm_forward(middle, norm_gains[1], norm_shifts[1], members)
    act_two = swish(pre_two).astype(jnp.bfloat16).reshape(grid_shape)
    branch, taps_two = conv_forward(act_two, row_mask, conv_weights[1], conv_biases[1])
    residual = inputs + branch
    normed_three, inverse_three, pre_three = norm_forward(
        residual, norm_gains[2], norm_shifts[2], members
    )
    attn_input = pre_three.astype(jnp.bfloat16)
    mixed = jnp.dot(attn_input, qkv_weight, preferred_element_type=jnp.float32)
    queries = (mixed[:, :channels] + qv_bias[0]).astype(jnp.bfloat16)
    key_rows = mixed[:, channels : 2 * channels].astype(jnp.bfloat16)
    value_rows = (mixed[:, 2 * channels :] + qv_bias[1]).astype(jnp.bfloat16)
    running_max = jnp.full((pixels,), masked_score, jnp.float32)
    key_piece = lax.all_gather(key_rows, "height", axis=0, tiled=True)
    value_piece = lax.all_gather(value_rows, "height", axis=0, tiled=True)
    scores = (
        lax.dot_general(
            queries, key_piece, (((1,), (1,)), ((), ())), preferred_element_type=jnp.float32
        )
        * score_scale
    )
    same_tile = query_ids[:, None] == key_ids[None, :]
    scores = jnp.where(same_tile, scores, masked_score)
    new_max = jnp.maximum(running_max, jnp.max(scores, axis=1))
    weights = jnp.where(same_tile, jnp.exp(scores - new_max[:, None]), 0.0)
    summed_out = jnp.dot(
        weights.astype(jnp.bfloat16), value_piece, preferred_element_type=jnp.float32
    )
    total_weight = jnp.sum(weights, axis=1)
    log_total = new_max + jnp.log(total_weight)
    attended = summed_out / total_weight[:, None]
    attended_low = attended.astype(jnp.bfloat16)
    output = (
        residual
        + jnp.dot(attended_low, proj_weight, preferred_element_type=jnp.float32)
        + proj_bias
    )
    out_grad = cotangent[0].reshape(pixels, channels)
    out_grad_full = out_grad.astype(jnp.float32)
    proj_grad = lax.dot_general(
        attended_low, out_grad, (((0,), (0,)), ((), ())), preferred_element_type=jnp.float32
    )
    proj_bias_grad = jnp.sum(out_grad_full, axis=0)
    attended_grad = lax.dot_general(
        out_grad, proj_weight, (((1,), (1,)), ((), ())), preferred_element_type=jnp.float32
    ).astype(jnp.bfloat16)
    row_dots = jnp.sum(attended_grad.astype(jnp.float32) * attended, axis=1)
    block_rows = pixels * min(height_size, 8)
    zero_block = jnp.zeros((pixels, channels), jnp.float32)
    key_all, value_all = (
        lax.all_gather(key_rows, "height", axis=0, tiled=True),
        lax.all_gather(value_rows, "height", axis=0, tiled=True),
    )
    query_all, grad_all = (
        lax.all_gather(queries, "height", axis=0, tiled=True),
        lax.all_gather(attended_grad, "height", axis=0, tiled=True),
    )
    total_all, dots_all = (
        lax.all_gather(log_total, "height", axis=0, tiled=True),
        lax.all_gather(row_dots, "height", axis=0, tiled=True),
    )

    def own_query_step(running, block_index):
        offset = block_index * block_rows
        key_part = take_rows(key_all, offset, block_rows)
        rounded, score_grad = score_grads(
            queries,
            attended_grad,
            log_total,
            row_dots,
            query_ids,
            key_part,
            take_rows(value_all, offset, block_rows),
            take_rows(key_ids, offset, block_rows),
            score_scale,
        )
        return (
            running
            + jnp.dot(score_grad, key_part, preferred_element_type=jnp.float32) * score_scale,
            None,
        )

    def own_key_step(running, block_index):
        offset = block_index * block_rows
        query_part = take_rows(query_all, offset, block_rows)
        grad_part = take_rows(grad_all, offset, block_rows)
        rounded, score_grad = score_grads(
            query_part,
            grad_part,
            take_rows(total_all, offset, block_rows),
            take_rows(dots_all, offset, block_rows),
            take_rows(key_ids, offset, block_rows),
            key_rows,
            value_rows,
            query_ids,
            score_scale,
        )
        key_part = (
            lax.dot_general(
                score_grad, query_part, (((0,), (0,)), ((), ())), preferred_element_type=jnp.float32
            )
            * score_scale
        )
        value_part = lax.dot_general(
            rounded, grad_part, (((0,), (0,)), ((), ())), preferred_element_type=jnp.float32
        )
        return ((running[0] + key_part, running[1] + value_part), None)

    block_count = key_all.shape[0] // block_rows
    query_grad, unused_one = lax.scan(own_query_step, zero_block, jnp.arange(block_count))
    (key_grad, value_grad), unused_two = lax.scan(
        own_key_step, (zero_block, zero_block), jnp.arange(block_count)
    )
    query_low = query_grad.astype(jnp.bfloat16)
    key_low = key_grad.astype(jnp.bfloat16)
    value_low = value_grad.astype(jnp.bfloat16)
    stacked_grad = jnp.concatenate([query_low, key_low, value_low], axis=1)
    qkv_grad = lax.dot_general(
        attn_input, stacked_grad, (((0,), (0,)), ((), ())), preferred_element_type=jnp.float32
    )
    qv_grad = jnp.stack(
        [
            jnp.sum(query_low.astype(jnp.float32), axis=0),
            jnp.sum(value_low.astype(jnp.float32), axis=0),
        ]
    )
    normed_grad = lax.dot_general(
        stacked_grad, qkv_weight, (((1,), (1,)), ((), ())), preferred_element_type=jnp.float32
    )
    back_three, gain_three, shift_three = norm_backward(
        normed_grad, normed_three, inverse_three, norm_gains[2], members
    )
    residual_grad = out_grad_full + back_three
    grad_two = residual_grad.astype(jnp.bfloat16).reshape(grid_shape)
    act_two_grad, weight_two_grad, bias_two_grad = conv_backward(
        grad_two, row_mask, conv_weights[1], taps_two
    )
    middle_grad, gain_two, shift_two = norm_backward(
        act_two_grad * swish_slope(pre_two), normed_two, inverse_two, norm_gains[1], members
    )
    grad_one = middle_grad.astype(jnp.bfloat16).reshape(grid_shape)
    act_one_grad, weight_one_grad, bias_one_grad = conv_backward(
        grad_one, row_mask, conv_weights[0], taps_one
    )
    input_back, gain_one, shift_one = norm_backward(
        act_one_grad * swish_slope(pre_one), normed_one, inverse_one, norm_gains[0], members
    )
    input_grad = residual_grad + input_back
    conv_grad = jnp.stack([weight_one_grad, weight_two_grad])
    conv_part = lax.psum_scatter(conv_grad, "height", scatter_dimension=4, tiled=True)
    conv_part = lax.psum_scatter(
        conv_part.astype(jnp.bfloat16), "canvas", scatter_dimension=3, tiled=True
    ).astype(jnp.float32)
    summed = lax.psum(
        (
            jnp.stack([gain_one, gain_two, gain_three]),
            jnp.stack([shift_one, shift_two, shift_three]),
            jnp.stack([bias_one_grad, bias_two_grad]),
            qkv_grad,
            qv_grad,
            proj_grad,
            proj_bias_grad,
        ),
        ("canvas", "height"),
    )
    return (
        output.astype(jnp.bfloat16).reshape((1,) + grid_shape),
        input_grad.astype(jnp.bfloat16).reshape((1,) + grid_shape),
        summed[0],
        summed[1],
        conv_part,
        summed[2],
        summed[3],
        summed[4],
        summed[5],
        summed[6],
    )


def fold(block):
    rows, width = block.shape
    return jnp.sum(block.reshape(rows // 8, 8, width), axis=0)


def group_lanes(block, group):
    lane = lax.broadcasted_iota(jnp.int32, block.shape, 1)
    width = block.shape[1]
    step = 1
    while step < group:
        above = pltpu.roll(block, step, 1)
        below = pltpu.roll(block, width - step, 1)
        block = block + jnp.where((lane & step) != 0, above, below)
        step *= 2
    return block


def group_mean(partial, members):
    spread = group_lanes(partial, partial.shape[1] // GROUPS)
    return jnp.sum(spread, axis=0, keepdims=True) * (1.0 / members)


def widen(block, width):
    return jnp.concatenate([block] * (width // block.shape[1]), axis=1)


def each_block(pixels, block, body, carry=0):
    def step(index, carry):
        return body(pl.ds(pl.multiple_of(index * block, block), block), carry)

    return lax.fori_loop(0, pixels // block, step, carry)


def each_chunk(pixels, body, carry):
    return each_block(pixels, CHUNK, body, carry)


def aligned(start, step):
    return start if isinstance(start, int) else pl.multiple_of(start, step)


class RunningStats:
    def __init__(self, channels):
        self.width = channels // GROUPS
        self.reference = None
        self.sums = self.squares = jnp.zeros((8, channels), jnp.float32)

    def add(self, block):
        if self.reference is None:
            self.reference = group_mean(block[0:8], 8.0 * self.width)
        offset = block - self.reference
        self.sums = self.sums + fold(offset)
        self.squares = self.squares + fold(offset * offset)

    def finish(self, pixels):
        both = group_lanes(jnp.concatenate([self.sums, self.squares], axis=0), self.width)
        share = 1.0 / (pixels * self.width)
        offset = column_total(both[0:8]) * share
        variance = column_total(both[8:16]) * share - offset * offset
        return self.reference + offset, lax.rsqrt(jnp.maximum(variance, 0.0) + epsilon)


def put_taps(taps_ref, block, rows, cols):
    count, channels = block.shape
    place = lax.broadcasted_iota(jnp.int32, block.shape, 0) & (cols - 1)
    left = jnp.where(place == 0, 0.0, pltpu.roll(block, 1, 0))
    right = jnp.where(place == cols - 1, 0.0, pltpu.roll(block, count - 1, 0))
    inner = pl.ds(aligned(rows.start + cols, cols), count)
    taps_ref[inner, 0:channels] = left.astype(jnp.bfloat16)
    taps_ref[inner, channels : 2 * channels] = block.astype(jnp.bfloat16)
    taps_ref[inner, 2 * channels :] = right.astype(jnp.bfloat16)


def clear_edges(taps_ref, cols):
    edge = jnp.zeros((cols, taps_ref.shape[1]), taps_ref.dtype)
    taps_ref[0:cols, :] = edge
    taps_ref[taps_ref.shape[0] - cols :, :] = edge


def begin_conv(taps_ref, product, total_ref, fill, first, cols):
    for start in range(0, total_ref.shape[0], FILL_ROWS):
        for inner in range(start, start + FILL_ROWS, CHUNK):
            fill(pl.ds(inner, CHUNK))
        rows = pl.ds(start, FILL_ROWS)
        total_ref[rows, :] = first(rows, product(taps_ref, pl.ds(start + cols, FILL_ROWS), 1))


def add_rows(taps_ref, product, mask_ref, total_ref, row_tap, last, cols, old_ref=None):
    pixels, channels = total_ref.shape
    old_ref = total_ref if old_ref is None else old_ref

    def step(rows, shifted):
        part = product(taps_ref, shifted, row_tap)
        mask = widen(mask_ref[row_tap // 2, rows, :], channels)
        value = old_ref[rows, :] + mask * part
        total_ref[rows, :] = value if last is None else last(rows, value)

    block = 2 * FILL_ROWS if last is None else FILL_ROWS
    for start in range(0, pixels, block):
        step(pl.ds(start, block), pl.ds(start + row_tap * cols, block))


def run_conv(taps_ref, product, mask_ref, total_ref, fill, first, last, cols):
    begin_conv(taps_ref, product, total_ref, fill, first, cols)
    add_rows(taps_ref, product, mask_ref, total_ref, 0, None, cols)
    add_rows(taps_ref, product, mask_ref, total_ref, 2, last, cols)


def product_forward(weight_ref):
    channels = weight_ref.shape[-1]

    def product(taps_ref, shifted, row_tap):
        return jnp.dot(
            taps_ref[shifted, :],
            weight_ref[row_tap].reshape(3 * channels, channels),
            preferred_element_type=jnp.float32,
        )

    return product


def product_backward(weight_ref):
    def product(taps_ref, shifted, row_tap):
        return lax.dot_general(
            taps_ref[shifted, :],
            weight_ref[row_tap],
            (((1,), (1,)), ((), ())),
            preferred_element_type=jnp.float32,
        )

    return product


def activation(read, mean, inverse, gain, shift, act_ref, taps_ref, cols):
    scale, offset = 0.5 * inverse * gain, 0.5 * shift

    def fill(rows):
        half = (read(rows) - mean) * scale + offset
        act = half * (1.0 + jnp.tanh(half))
        act_ref[rows, :] = act.astype(jnp.bfloat16)
        put_taps(taps_ref, act, rows, cols)

    return fill


def back_means(sums, gain, pixels):
    channels = gain.shape[1]
    members = float(pixels * (channels // GROUPS))
    return group_mean(sums[0] * gain, members), group_mean(sums[1] * gain, members)


def column_total(partial):
    return jnp.sum(partial, axis=0, keepdims=True)


def weight_part(act_ref, narrow, lanes_ref, flip_ref, columns_ref, part_ref, cols):
    pixels, channels = act_ref.shape
    height = lax.axis_index("height")
    share = NARROW // 2
    flip_ref[...] = narrow.T
    own = pl.ds(pl.multiple_of((height % 2) * share, share), share)
    grad = flip_ref[own, :].astype(jnp.float32)
    column = lax.broadcasted_iota(jnp.int32, grad.shape, 1) & (cols - 1)
    for col_tap in range(3):
        shifted = grad
        if col_tap == 0:
            shifted = jnp.where(column == cols - 1, 0.0, pltpu.roll(grad, pixels - 1, 1))
        elif col_tap == 2:
            shifted = jnp.where(column == 0, 0.0, pltpu.roll(grad, 1, 1))
        for row_tap in range(3):
            tap = 3 * row_tap + col_tap
            place = slice(tap * share, (tap + 1) * share)
            if row_tap == 1:
                columns_ref[place, :] = shifted.astype(jnp.bfloat16)
                continue
            side, turn = (0, pixels - cols) if row_tap == 0 else (1, cols)
            masked = (shifted * lanes_ref[side : side + 1, :]).astype(jnp.bfloat16)
            columns_ref[place, :] = pltpu.roll(masked, turn, 1)
    part_ref[...] = jnp.dot(
        columns_ref[...], act_ref[...], preferred_element_type=jnp.float32
    ).astype(jnp.bfloat16)


def begin_back(grad_ref, weights_ref, mask_ref, taps_ref, total_ref, cols):
    clear_edges(taps_ref, cols)

    def fill(rows):
        put_taps(taps_ref, grad_ref[rows, :].astype(jnp.float32), rows, cols)

    product = product_backward(weights_ref)
    begin_conv(taps_ref, product, total_ref, fill, lambda rows, part: part, cols)
    add_rows(taps_ref, product, mask_ref, total_ref, 0, None, cols)


def finish_back(
    weights_ref, mask_ref, taps_ref, total_ref, read, table_ref, which, cols, old_ref=None
):
    mean, inverse, gain, shift = norm_rows(table_ref, which)
    scale, offset = 0.5 * inverse * gain, 0.5 * shift
    sums = []

    def slope(rows, value):
        centered = read(rows) - mean
        half = centered * scale + offset
        turn = jnp.tanh(half)
        double = value * ((1.0 + turn) * (1.0 + half * (1.0 - turn)))
        sums.append((fold(double), fold(double * centered)))
        return double

    add_rows(
        taps_ref, product_backward(weights_ref), mask_ref, total_ref, 2, slope, cols, old_ref
    )
    plain, cross = sum(pair[0] for pair in sums), sum(pair[1] for pair in sums)
    return 0.5 * plain, 0.5 * inverse * cross


def norm_back(total_ref, double, sums, read, table_ref, which, pixels, scales_ref=None):
    mean, inverse, gain, shift = norm_rows(table_ref, which)
    mean_grad, mean_cross = back_means(sums, gain, pixels)
    slope = inverse * gain * (0.5 if double else 1.0)
    level, tilt = inverse * mean_grad, inverse * inverse * mean_cross
    if scales_ref is not None:
        for row, scales in enumerate((mean, slope, level, tilt)):
            scales_ref[row : row + 1, :] = scales

    def back(rows, inner):
        return total_ref[inner, :] * slope - level - (read(rows) - mean) * tilt

    return back


def own_lanes():
    block = lax.axis_index("height") // 2
    return pl.ds(pl.multiple_of(block * NARROW, NARROW), NARROW)


def narrow_back(total_ref, value_ref, scales_ref):
    lanes = own_lanes()
    mean, slope, level, tilt = (scales_ref[row : row + 1, lanes] for row in range(4))
    return total_ref[:, lanes] * slope - level - (value_ref[:, lanes] - mean) * tilt


def turn_kernel(
    grad_ref, mask_ref, weights_ref, middle_ref, table_ref, total_ref, sums_ref, taps_ref, *, cols
):
    begin_back(grad_ref, weights_ref.at[1], mask_ref, taps_ref, total_ref, cols)
    sums_ref[0:8, :], sums_ref[8:16, :] = finish_back(
        weights_ref.at[1],
        mask_ref,
        taps_ref,
        total_ref,
        lambda rows: middle_ref[rows, :],
        table_ref,
        1,
        cols,
    )


def norm_rows(table_ref, which):
    picks = (2 * which, 2 * which + 1, 6 + which, 9 + which)
    return tuple(table_ref[pick : pick + 1, :] for pick in picks)


def build_masks(ids_ref, mask_ref, lanes_ref, id_rows_ref, id_cols_ref, cols):
    rows = ids_ref.shape[1]

    def one_row(row, carry):
        here = ids_ref[0, row]
        place = pl.ds(pl.multiple_of(row * cols, cols), cols)
        id_rows_ref[place, :] = jnp.full((cols, LANES), here, jnp.int32)
        for side, other in ((0, row - 1), (1, row + 1)):
            inside = jnp.logical_and(other >= 0, other < rows)
            other_id = ids_ref[0, jnp.clip(other, 0, rows - 1)]
            same = jnp.where(jnp.logical_and(inside, other_id == here), 1.0, 0.0)
            mask_ref[side, place, :] = jnp.full((cols, LANES), same, jnp.float32)
        return carry

    lax.fori_loop(0, rows, one_row, 0)
    lane = lax.broadcasted_iota(jnp.int32, (8, LANES), 1)
    each = LANES // cols
    for block in range(rows // each):
        ids = jnp.full((8, LANES), ids_ref[0, block * each], jnp.int32)
        for step in range(1, each):
            ids = jnp.where(lane >= step * cols, ids_ref[0, block * each + step], ids)
        id_cols_ref[:, block * LANES : (block + 1) * LANES] = ids
    ids = id_cols_ref[...].astype(jnp.float32)
    pixels = ids.shape[1]
    pixel = lax.broadcasted_iota(jnp.int32, ids.shape, 1)
    above = jnp.where(pixel < cols, -1.0, pltpu.roll(ids, cols, 1))
    below = jnp.where(pixel >= pixels - cols, -1.0, pltpu.roll(ids, pixels - cols, 1))
    lanes_ref[0:1, :] = jnp.where(above == ids, 1.0, 0.0)[0:1]
    lanes_ref[1:2, :] = jnp.where(below == ids, 1.0, 0.0)[0:1]


def place_pieces(pieces, whole_ref, sems):
    own_pixels = whole_ref.shape[0] // len(pieces)
    height = lax.axis_index("height")
    copies = []
    for place, piece in enumerate(pieces):
        start = pl.multiple_of((height ^ place) * own_pixels, own_pixels)
        rows = pl.ds(start, own_pixels)
        copies.append(pltpu.make_async_copy(piece, whole_ref.at[rows, :], sems.at[place]))
    return copies


def hold_kernel(
    ids_hbm,
    gains_hbm,
    shifts_hbm,
    biases_hbm,
    weights_hbm,
    qkv_hbm,
    proj_hbm,
    qv_bias_hbm,
    proj_bias_hbm,
    weights_ref,
    turned_ref,
    qkv_ref,
    proj_ref,
    table_ref,
    mask_ref,
    lanes_ref,
    id_rows_ref,
    id_cols_ref,
    ids_ref,
    gains_ref,
    shifts_ref,
    biases_ref,
    qv_bias_ref,
    proj_bias_ref,
    sems,
    *,
    cols,
):
    channels = weights_ref.shape[-1]
    small = [
        (ids_hbm, ids_ref),
        (gains_hbm, gains_ref),
        (shifts_hbm, shifts_ref),
        (biases_hbm, biases_ref),
        (qv_bias_hbm, qv_bias_ref),
        (proj_bias_hbm, proj_bias_ref),
    ]
    large = [(weights_hbm, weights_ref), (qkv_hbm, qkv_ref), (proj_hbm, proj_ref)]
    for which in range(2):
        for row_tap in range(3):
            for col_tap in range(3):
                place = slice(col_tap * channels, (col_tap + 1) * channels)
                large.append(
                    (
                        weights_hbm.at[which, 2 - row_tap, 2 - col_tap],
                        turned_ref.at[which, row_tap, :, place],
                    )
                )
    copies = [
        pltpu.make_async_copy(source, target, sems.at[index])
        for index, (source, target) in enumerate(small + large)
    ]
    for copy in copies:
        copy.start()
    for copy in copies[: len(small)]:
        copy.wait()
    build_masks(ids_ref, mask_ref, lanes_ref, id_rows_ref, id_cols_ref, cols)
    table_ref[6:9, :] = gains_ref[...]
    table_ref[9:12, :] = shifts_ref[...]
    table_ref[12:14, :] = biases_ref[...]
    table_ref[14:16, :] = qv_bias_ref[...]
    table_ref[16:17, :] = proj_bias_ref[...]
    for copy in copies[len(small) :]:
        copy.wait()


def conv_kernel(*refs, cols, count):
    pieces, refs = refs[:count], refs[count:]
    (
        weights_ref,
        params_ref,
        mask_ref,
        features_ref,
        act_one_ref,
        middle_ref,
        act_two_ref,
        residual_ref,
        table_ref,
        own_ref,
        taps_ref,
        sem,
    ) = refs
    pixels, channels = features_ref.shape
    wide = jnp.float32
    own_copy = pltpu.make_async_copy(pieces[0], own_ref, sem)
    own_copy.start()
    table_ref[...] = params_ref[...]
    clear_edges(taps_ref, cols)

    def read_input(rows):
        return features_ref[rows, :].astype(wide)

    def read_middle(rows):
        return middle_ref[rows, :]

    height = lax.axis_index("height")
    own_pixels = pixels // count
    seen = RunningStats(channels)
    for place in list(range(1, count)) + [0]:
        if place == 0:
            own_copy.wait()
        piece = (pieces[place] if place else own_ref)[...]
        start = pl.multiple_of((height ^ place) * own_pixels, own_pixels)
        features_ref[pl.ds(start, own_pixels), :] = piece
        seen.add(piece.astype(wide))
    table_ref[0:1, :], table_ref[1:2, :] = seen.finish(pixels)
    seen = RunningStats(channels)

    def keep(rows, value):
        seen.add(value)
        return value

    run_conv(
        taps_ref,
        product_forward(weights_ref.at[0]),
        mask_ref,
        middle_ref,
        activation(read_input, *norm_rows(table_ref, 0), act_one_ref, taps_ref, cols),
        lambda rows, part: part + table_ref[12:13, :],
        keep,
        cols,
    )
    table_ref[2:3, :], table_ref[3:4, :] = seen.finish(pixels)
    seen = RunningStats(channels)
    run_conv(
        taps_ref,
        product_forward(weights_ref.at[1]),
        mask_ref,
        residual_ref,
        activation(read_middle, *norm_rows(table_ref, 1), act_two_ref, taps_ref, cols),
        lambda rows, part: part + (read_input(rows) + table_ref[13:14, :]),
        keep,
        cols,
    )
    table_ref[4:5, :], table_ref[5:6, :] = seen.finish(pixels)


def score_kernel(
    qkv_ref,
    proj_ref,
    residual_ref,
    table_ref,
    id_rows_ref,
    id_cols_ref,
    normed_ref,
    query_ref,
    key_ref,
    value_ref,
    soft_ref,
    out_flip_ref,
    output_ref,
    value_flip_ref,
    *scores_refs,
    score_scale,
):
    pixels, channels = residual_ref.shape
    own_pixels = output_ref.shape[0]
    wide = jnp.float32
    exponent = score_scale * 1.4426950408889634
    mean, inverse, gain, shift = norm_rows(table_ref, 2)
    scale = inverse * gain

    def normalise(start):
        rows = slice(start, start + KEY_ROWS)
        normed = (residual_ref[rows, :] - mean) * scale + shift
        normed_ref[rows, :] = normed.astype(jnp.bfloat16)

    def project(start):
        rows = slice(start, start + KEY_ROWS)
        normed = normed_ref[rows, :]
        query_ref[rows, :] = (
            jnp.dot(normed, qkv_ref[:, 0:channels], preferred_element_type=wide)
            + table_ref[14:15, :]
        ).astype(jnp.bfloat16)
        key_ref[rows, :] = jnp.dot(
            normed, qkv_ref[:, channels : 2 * channels], preferred_element_type=wide
        ).astype(jnp.bfloat16)
        values = (
            jnp.dot(normed, qkv_ref[:, 2 * channels :], preferred_element_type=wide)
            + table_ref[15:16, :]
        ).astype(jnp.bfloat16)
        value_ref[rows, :] = values
        value_flip_ref[:, rows] = values.T

    normalise(0)
    for start in range(0, pixels, KEY_ROWS):
        if start + KEY_ROWS < pixels:
            normalise(start + KEY_ROWS)
        project(start)
    block = scores_refs[0].shape[1]
    steps = range(0, pixels, KEY_ROWS)

    def score(index):
        rows = slice(index * block, (index + 1) * block)
        for start in steps:
            keys = slice(start, start + KEY_ROWS)
            scores = lax.dot_general(
                key_ref[keys, :],
                query_ref[rows, :],
                (((1,), (1,)), ((), ())),
                preferred_element_type=wide,
            )
            same = widen(id_rows_ref[keys, :], block) == id_cols_ref[0:1, rows]
            scores_refs[index][keys, :] = jnp.where(same, scores, masked_score)

    def soften(index):
        rows = slice(index * block, (index + 1) * block)
        scores_ref = scores_refs[index]
        peak = jnp.full((8, block), masked_score, wide)
        for start in steps:
            scores = scores_ref[start : start + KEY_ROWS, :]
            peak = jnp.maximum(peak, jnp.max(scores.reshape(-1, 8, block), axis=0))
        peak = jnp.max(peak, axis=0, keepdims=True)
        total = jnp.zeros((8, block), wide)
        for start in steps:
            keys = slice(start, start + KEY_ROWS)
            powers = jnp.exp2((scores_ref[keys, :] - peak) * exponent)
            scores_ref[keys, :] = powers
            total = total + fold(powers)
        share = 1.0 / column_total(total)
        for start in steps:
            keys = slice(start, start + KEY_ROWS)
            soft_ref[keys, rows] = (scores_ref[keys, :] * share).astype(jnp.bfloat16)

    score(0)
    for index in range(len(scores_refs)):
        if index + 1 < len(scores_refs):
            score(index + 1)
        soften(index)

    def collect(rows, carry):
        out_flip_ref[rows, :] = jnp.dot(
            value_flip_ref[rows, :], soft_ref[...], preferred_element_type=wide
        ).astype(jnp.bfloat16)
        return carry

    each_block(channels, channels // 2, collect)
    height = lax.axis_index("height")
    own = pl.ds(pl.multiple_of(height * own_pixels, own_pixels), own_pixels)
    output_ref[...] = (
        residual_ref[own, :]
        + lax.dot_general(
            out_flip_ref[:, own],
            proj_ref[...],
            (((0,), (0,)), ((), ())),
            preferred_element_type=wide,
        )
        + table_ref[16:17, :]
    ).astype(jnp.bfloat16)


def own_quarter():
    height = lax.axis_index("height")
    return (height & 1) * 2 + ((height >> 1) & 1)


def send_order(source_ref, targets, axis, share):
    me = lax.axis_index("canvas")
    for step, target in enumerate(targets):
        place = pl.ds(pl.multiple_of((me ^ step) * share, share), share)
        target[...] = source_ref[place, :] if axis == 0 else source_ref[:, place]


def attention_kernel(
    proj_ref,
    normed_ref,
    query_ref,
    key_ref,
    value_ref,
    soft_ref,
    out_flip_ref,
    *refs,
    score_scale,
    count,
):
    pieces, (grad_ref, packed_ref, sums_ref), refs = (
        refs[:count],
        refs[count : count + 3],
        refs[count + 3 :],
    )
    pixels, channels = normed_ref.shape
    blocks = pixels // SCORE_ROWS
    grads_refs, refs = refs[-blocks:], refs[:-blocks]
    *mixed_refs, mixed_ref, key_flip_ref, back_ref, score_grad_ref, flip_ref, sems = refs
    wide = jnp.float32
    copies = place_pieces(pieces, grad_ref, sems)
    for copy in copies:
        copy.start()
    quarter = channels // 4
    own = pl.ds(pl.multiple_of(own_quarter() * quarter, quarter), quarter)
    flip_ref[...] = normed_ref[:, own].T
    key_flip_ref[...] = key_ref[...].T
    for copy in copies:
        copy.wait()
    block, count = SCORE_ROWS, blocks
    steps = range(0, pixels, KEY_ROWS)

    def block_rows(index):
        return slice(index * block, (index + 1) * block)

    for index in range(count):
        back_ref[block_rows(index), :] = lax.dot_general(
            grad_ref[block_rows(index), :],
            proj_ref[...],
            (((1,), (1,)), ((), ())),
            preferred_element_type=wide,
        ).astype(jnp.bfloat16)

    def weigh(index):
        total = jnp.zeros((8, block), wide)
        for start in steps:
            keys = slice(start, start + KEY_ROWS)
            weight_grad = lax.dot_general(
                value_ref[keys, :],
                back_ref[block_rows(index), :],
                (((1,), (1,)), ((), ())),
                preferred_element_type=wide,
            )
            grads_refs[index][keys, :] = weight_grad
            total = total + fold(soft_ref[keys, block_rows(index)].astype(wide) * weight_grad)
        return column_total(total)

    def slope(index, dots):
        for start in steps:
            keys = slice(start, start + KEY_ROWS)
            weights = soft_ref[keys, block_rows(index)].astype(wide)
            score_grad_ref[keys, block_rows(index)] = (
                weights * (grads_refs[index][keys, :] - dots)
            ).astype(jnp.bfloat16)

    dots = weigh(0)
    for index in range(count):
        now, rows = dots, block_rows(index)
        if index + 1 < count:
            dots = weigh(index + 1)
        slope(index, now)
        packed_ref[rows, 2 * channels :] = jnp.dot(
            soft_ref[rows, :], back_ref[...], preferred_element_type=wide
        ).astype(jnp.bfloat16)
        query_grad = jnp.dot(
            key_flip_ref[...], score_grad_ref[:, rows], preferred_element_type=wide
        )
        packed_ref[rows, 0:channels] = (query_grad * score_scale).astype(jnp.bfloat16).T
    for index in range(count):
        rows = block_rows(index)
        packed_ref[rows, channels : 2 * channels] = (
            jnp.dot(score_grad_ref[rows, :], query_ref[...], preferred_element_type=wide)
            * score_scale
        ).astype(jnp.bfloat16)

    def pack(rows, carry):
        return (
            carry[0] + fold(packed_ref[rows, 0:channels].astype(wide)),
            carry[1] + fold(packed_ref[rows, 2 * channels :].astype(wide)),
            carry[2] + fold(grad_ref[rows, :].astype(wide)),
        )

    zeros = jnp.zeros((8, channels), wide)
    totals = zeros, zeros, zeros
    for start in range(0, pixels, CHUNK):
        totals = pack(pl.ds(start, CHUNK), totals)
    sums_ref[...] = jnp.zeros(sums_ref.shape, wide)
    for row, total in enumerate(totals):
        sums_ref[8 + row : 9 + row, :] = column_total(total)
    mixed_ref[:, 0 : 3 * channels] = jnp.dot(
        flip_ref[...], packed_ref[...], preferred_element_type=wide
    ).astype(jnp.bfloat16)
    mixed_ref[:, 3 * channels :] = jnp.dot(
        out_flip_ref[own, :], grad_ref[...], preferred_element_type=wide
    ).astype(jnp.bfloat16)
    send_order(mixed_ref, mixed_refs, 0, quarter // len(mixed_refs))


def third_kernel(
    qkv_ref,
    grad_ref,
    packed_ref,
    residual_ref,
    table_ref,
    act_two_ref,
    lanes_ref,
    old_sums_ref,
    residual_grad_ref,
    grad_two_ref,
    sums_ref,
    keep_ref,
    send_ref,
    total_ref,
    flip_ref,
    columns_ref,
    part_ref,
    *,
    cols,
):
    pixels, channels = residual_ref.shape
    block = FILL_ROWS
    wide = jnp.float32
    mean, inverse, gain, shift = norm_rows(table_ref, 2)
    zeros = jnp.zeros((8, channels), wide)

    sums = (zeros, zeros)
    for start in range(0, pixels, block):
        rows = pl.ds(start, block)
        normed_grad = lax.dot_general(
            packed_ref[rows, :], qkv_ref[...], (((1,), (1,)), ((), ())), preferred_element_type=wide
        )
        total_ref[rows, :] = normed_grad
        centered = residual_ref[rows, :] - mean
        sums = sums[0] + fold(normed_grad), sums[1] + fold(normed_grad * centered)
    sums = sums[0], sums[1] * inverse
    sums_ref[...] = old_sums_ref[...]
    sums_ref[5:6, :] = column_total(sums[1])
    sums_ref[6:7, :] = column_total(sums[0])
    back = norm_back(
        total_ref, False, sums, lambda rows: residual_ref[rows, :], table_ref, 2, pixels
    )

    def finish(rows, carry):
        total = grad_ref[rows, :].astype(wide) + back(rows, rows)
        residual_grad_ref[rows, :] = total
        low = total.astype(jnp.bfloat16)
        grad_two_ref[rows, :] = low
        return carry + fold(low.astype(wide))

    sums_ref[7:8, :] = column_total(each_chunk(pixels, finish, zeros))
    narrow = grad_two_ref[:, own_lanes()]
    weight_part(act_two_ref, narrow, lanes_ref, flip_ref, columns_ref, part_ref, cols)
    keep_half(part_ref, 2, 1, keep_ref, send_ref)


def second_kernel(
    total_ref,
    partial_ref,
    middle_ref,
    table_ref,
    act_one_ref,
    lanes_ref,
    old_sums_ref,
    grad_one_ref,
    sums_ref,
    keep_ref,
    send_ref,
    flip_ref,
    columns_ref,
    part_ref,
    scales_ref,
    *,
    cols,
):
    pixels, channels = middle_ref.shape
    sums = partial_ref[0:8, :], partial_ref[8:16, :]
    back = norm_back(
        total_ref, True, sums, lambda rows: middle_ref[rows, :], table_ref, 1, pixels, scales_ref
    )
    narrow = narrow_back(total_ref, middle_ref, scales_ref).astype(jnp.bfloat16)
    weight_part(act_one_ref, narrow, lanes_ref, flip_ref, columns_ref, part_ref, cols)
    sums_ref[...] = old_sums_ref[...]
    sums_ref[2:3, :] = column_total(sums[1])
    sums_ref[3:4, :] = column_total(sums[0])

    def finish(rows, carry):
        low = back(rows, rows).astype(jnp.bfloat16)
        grad_one_ref[rows, :] = low
        return carry + fold(low.astype(jnp.float32))

    zeros = jnp.zeros((8, channels), jnp.float32)
    sums_ref[4:5, :] = column_total(each_chunk(pixels, finish, zeros))
    keep_half(part_ref, 1, 2, keep_ref, send_ref)


def keep_half(part_ref, near, far, keep_ref, send_ref):
    me = lax.axis_index("canvas")
    rows, width = part_ref.shape[0], keep_ref.shape[1]
    for target_ref, flip in ((keep_ref, 0), (send_ref, near)):
        for slot in range(2):
            owner = me ^ flip ^ (slot * far)
            place = pl.ds(pl.multiple_of(owner * width, width), width)
            target_ref[slot * rows : (slot + 1) * rows, :] = part_ref[:, place]


def first_kernel(
    grad_one_ref,
    features_ref,
    table_ref,
    mask_ref,
    old_sums_ref,
    weights_ref,
    own_ref,
    sums_ref,
    partial_ref,
    total_ref,
    taps_ref,
    *,
    cols,
):
    def read(rows):
        return features_ref[rows, :].astype(jnp.float32)

    weights = weights_ref.at[0]
    begin_back(grad_one_ref, weights, mask_ref, taps_ref, total_ref, cols)
    sums = finish_back(weights, mask_ref, taps_ref, total_ref, read, table_ref, 0, cols)
    partial_ref[0:8, :], partial_ref[8:16, :] = sums
    sums_ref[...] = old_sums_ref[...]
    sums_ref[0:1, :] = column_total(sums[1])
    sums_ref[1:2, :] = column_total(sums[0])
    count = own_ref.shape[0]
    own = pl.ds(pl.multiple_of(lax.axis_index("height") * count, count), count)
    own_ref[...] = total_ref[own, :]


def own_kernel(
    own_ref, partial_ref, features_ref, residual_grad_ref, table_ref, input_grad_ref
):
    def read(rows):
        return features_ref[rows, :].astype(jnp.float32)

    sums = partial_ref[0:8, :], partial_ref[8:16, :]
    pixels = features_ref.shape[0]
    back = norm_back(own_ref, True, sums, read, table_ref, 0, pixels)
    count = own_ref.shape[0]
    own = pl.ds(pl.multiple_of(lax.axis_index("height") * count, count), count)
    total = residual_grad_ref[own, :] + back(own, slice(0, count))
    input_grad_ref[...] = total.astype(jnp.bfloat16)


def place_kernel(*refs):
    joints, packed_ref = refs[:-1], refs[-1]
    share = packed_ref.shape[0] // len(joints)
    me = lax.axis_index("canvas")
    for step, joint in enumerate(joints):
        place = pl.ds(pl.multiple_of((me ^ step) * share, share), share)
        packed_ref[place, :] = joint[...]


def spread_quarters(packed, flips, qkv_ref, proj_ref, qkv_hbm, proj_hbm, sems):
    quarter = packed[0].shape[0]
    inner = qkv_ref.shape[2]
    copies = []
    for index, packed_ref in enumerate(packed):
        owner = own_quarter() ^ flips[index]
        rows = pl.ds(pl.multiple_of(owner * quarter, quarter), quarter)
        qkv_ref[index] = packed_ref[:, 0:inner].astype(jnp.float32)
        proj_ref[index] = packed_ref[:, inner:].astype(jnp.float32)
        for which, (held, target) in enumerate(((qkv_ref, qkv_hbm), (proj_ref, proj_hbm))):
            copy = pltpu.make_async_copy(held.at[index], target.at[rows, :], sems.at[index, which])
            copy.start()
            copies.append(copy)
    return copies


def join_kernel(*refs):
    packed, (qkv_hbm, proj_hbm, qkv_ref, proj_ref, sems) = refs[:-5], refs[-5:]
    copies = spread_quarters(
        packed, range(len(packed)), qkv_ref, proj_ref, qkv_hbm, proj_hbm, sems
    )
    for copy in copies:
        copy.wait()


def halve_kernel(keep_ref, got_ref, hold_ref, send_ref):
    total = keep_ref[...].astype(jnp.float32) + got_ref[...].astype(jnp.float32)
    rows = hold_ref.shape[0]
    hold_ref[...] = total[0:rows]
    send_ref[0:rows, :] = total[rows:].astype(jnp.bfloat16)


def halve_sums_kernel(
    keep_one_ref,
    got_one_ref,
    keep_two_ref,
    got_two_ref,
    sums_ref,
    hold_ref,
    send_ref,
    hold_two_ref,
    send_two_ref,
):
    halve_kernel(keep_one_ref, got_one_ref, hold_ref, send_ref)
    halve_kernel(keep_two_ref, got_two_ref, hold_two_ref, send_two_ref)
    rows = hold_ref.shape[0]
    low = sums_ref[...].astype(jnp.bfloat16)
    count, width = low.shape
    for block in range(width // LANES):
        place = slice(rows + block * count, rows + (block + 1) * count)
        piece = low[:, block * LANES : (block + 1) * LANES]
        send_ref[place, :] = piece
        send_two_ref[place, :] = piece


def unpack_sums(got_ref, rows, count, width):
    blocks = [
        got_ref[start : start + count, :].astype(jnp.float32)
        for start in range(rows, rows + width // LANES * count, count)
    ]
    return jnp.concatenate(blocks, axis=1)


def sums_kernel(
    sums_ref,
    far_ref,
    hold_one_ref,
    got_one_ref,
    hold_two_ref,
    got_two_ref,
    share_ref,
    gains_ref,
    shifts_ref,
    conv_ref,
    qv_ref,
    bias_ref,
):
    rows = hold_one_ref.shape[0]
    for which, (hold_ref, got_ref) in enumerate(
        ((hold_one_ref, got_one_ref), (hold_two_ref, got_two_ref))
    ):
        total = hold_ref[...] + got_ref[0:rows, :].astype(jnp.float32)
        share_ref[which] = total.reshape(share_ref.shape[1:])
    total = sums_ref[...] + far_ref[...]
    for got_ref in (got_one_ref, got_two_ref):
        total = total + unpack_sums(got_ref, rows, *total.shape)
    for row, start in enumerate((0, 2, 5)):
        gains_ref[row : row + 1, :] = total[start : start + 1]
        shifts_ref[row : row + 1, :] = total[start + 1 : start + 2]
    conv_ref[0:1, :] = total[4:5]
    conv_ref[1:2, :] = total[7:8]
    qv_ref[...] = total[8:10]
    bias_ref[...] = total[10:11]


def call_kernel(kernel, outputs, scratch, operands, places, flops, limit, out_places=None, aliases={}):
    out_places = out_places or "v" * len(outputs)
    spaces = {
        "v": pl.BlockSpec(memory_space=pltpu.VMEM),
        "s": pl.BlockSpec(memory_space=pltpu.SMEM),
        "h": pl.BlockSpec(memory_space=pl.ANY),
        "o": pl.BlockSpec(memory_space=pltpu.VMEM),
        "a": pl.BlockSpec(memory_space=pl.ANY),
    }
    moved = 8 * flops // LANES
    held = {"v": pltpu.VMEM, "h": pltpu.HBM, "o": jax.ShapeDtypeStruct}
    operands = [
        pltpu.with_memory_space_constraint(array, pltpu.HBM) if place == "h" else array
        for array, place in zip(operands, places)
    ]
    return pl.pallas_call(
        kernel,
        out_shape=[held[place](*output) for output, place in zip(outputs, out_places)],
        in_specs=[spaces[place] for place in places],
        out_specs=[spaces[place] for place in out_places],
        scratch_shapes=scratch,
        input_output_aliases=aliases,
        compiler_params=pltpu.CompilerParams(vmem_limit_bytes=limit * 2**20),
        cost_estimate=pl.CostEstimate(flops=flops, bytes_accessed=moved, transcendentals=0),
    )(*operands)


def send_height(block, step):
    size = lax.axis_size("height")
    return lax.ppermute(block, "height", [(i, i ^ step) for i in range(size)])


def with_cores(blocks):
    return [piece for block in blocks for piece in (block, send_height(block, 1))]


def send_canvas(block, step):
    size = lax.axis_size("canvas")
    return lax.ppermute(block, "canvas", [(i, i ^ step) for i in range(size)])


def trade_canvas(pieces):
    return [pieces[0]] + [send_canvas(piece, step) for step, piece in enumerate(pieces) if step]


def whole_canvas(
    features,
    tile_ids,
    norm_gains,
    norm_shifts,
    conv_weights,
    conv_biases,
    qkv_weight,
    qv_bias,
    proj_weight,
    proj_bias,
    cotangent,
):
    height_size = lax.axis_size("height")
    canvas_size = lax.axis_size("canvas")
    local_rows, cols, channels = features.shape[1:]
    all_rows = tile_ids.shape[1]
    pixels = all_rows * cols
    own_pixels = local_rows * cols
    out_share = channels // height_size
    ci_share = channels // canvas_size
    quarter = channels // 4
    row_share = quarter // canvas_size
    low, wide = jnp.bfloat16, jnp.float32

    own_features = features.reshape(own_pixels, channels)
    own_grad = cotangent.reshape(own_pixels, channels)
    steps = range(2, height_size, 2)
    held_features = [own_features] + [send_height(own_features, step) for step in steps]
    plane = ((pixels, channels), low)
    plane_wide = ((pixels, channels), wide)
    sums_shape = ((16, channels), wide)
    mixed_shapes = [((row_share, 4 * channels), low)] * canvas_size
    taps = pltpu.VMEM((pixels + 2 * cols, 3 * channels), low)
    held_wide = pltpu.VMEM((pixels, channels), wide)
    flipped = pltpu.VMEM((channels, pixels), low)
    narrow = pltpu.VMEM((NARROW, pixels), low)
    columns = pltpu.VMEM((9 * out_share, pixels), low)
    part_held = pltpu.VMEM((9 * out_share, channels), low)
    sem = pltpu.SemaphoreType.DMA
    conv_flops = 2 * 9 * pixels * channels * channels
    dot_flops = 2 * pixels * channels * channels
    score_flops = 2 * pixels * pixels * channels
    scale = channels ** (-0.5)

    (
        held_conv,
        turned,
        held_qkv,
        held_proj,
        params,
        mask,
        lane_mask,
        id_rows,
        id_cols,
    ) = call_kernel(
        functools.partial(hold_kernel, cols=cols),
        [
            (conv_weights.shape, low),
            ((2, 3, channels, 3 * channels), low),
            (qkv_weight.shape, low),
            (proj_weight.shape, low),
            ((24, channels), wide),
            ((2, pixels, LANES), wide),
            ((8, pixels), wide),
            ((pixels, LANES), jnp.int32),
            ((8, pixels), jnp.int32),
        ],
        [
            pltpu.SMEM(tile_ids.shape, jnp.int32),
            pltpu.VMEM(norm_gains.shape, wide),
            pltpu.VMEM(norm_shifts.shape, wide),
            pltpu.VMEM(conv_biases.shape, wide),
            pltpu.VMEM(qv_bias.shape, wide),
            pltpu.VMEM((1, channels), wide),
            sem((27,)),
        ],
        [
            tile_ids,
            norm_gains,
            norm_shifts,
            conv_biases,
            conv_weights,
            qkv_weight,
            proj_weight,
            qv_bias,
            proj_bias.reshape(1, channels),
        ],
        "h" * 9,
        conv_flops,
        8,
    )
    held_features[1:] = [
        lax.optimization_barrier((params, block))[1] for block in held_features[1:]
    ]
    pieces = with_cores(held_features)
    far_grad, *pieces[4::2] = lax.optimization_barrier((own_grad, *held_features[2:]))
    held_grads = [own_grad, send_height(own_grad, 2)]
    held_grads[1], pieces[2] = lax.optimization_barrier((held_grads[1], held_features[1]))
    held_grads += [send_height(far_grad, step) for step in steps[1:]]

    all_features, act_one, middle, act_two, residual, table = call_kernel(
        functools.partial(conv_kernel, cols=cols, count=height_size),
        [plane, plane, plane_wide, plane, plane_wide, ((24, channels), wide)],
        [pltpu.VMEM((own_pixels, channels), low), taps, sem],
        [*pieces, held_conv, params, mask],
        "h" + "v" * (height_size + 2),
        2 * conv_flops,
        16,
    )
    residual, *held_grads = lax.optimization_barrier((residual, *held_grads))
    grad_pieces = with_cores(held_grads)
    normed, query, key, value, soft, out_flip, output = call_kernel(
        functools.partial(score_kernel, score_scale=scale),
        [
            plane,
            plane,
            plane,
            plane,
            ((pixels, pixels), low),
            ((channels, pixels), low),
            ((own_pixels, channels), low),
        ],
        [
            flipped,
            *[pltpu.VMEM((pixels, SCORE_ROWS), wide)] * (pixels // SCORE_ROWS),
        ],
        [
            held_qkv,
            held_proj,
            residual,
            table,
            id_rows,
            id_cols,
        ],
        "vvvvvv",
        3 * dot_flops + 2 * score_flops,
        20,
        "v" * 6 + "o",
    )
    normed, *grad_pieces = lax.optimization_barrier((normed, *grad_pieces))
    all_grad, packed, sums, *mixed = call_kernel(
        functools.partial(attention_kernel, score_scale=scale, count=height_size),
        [plane, ((pixels, 3 * channels), low), sums_shape, *mixed_shapes],
        [
            pltpu.VMEM((quarter, 4 * channels), low),
            flipped,
            pltpu.VMEM((pixels, channels), low),
            pltpu.VMEM((pixels, pixels), low),
            pltpu.VMEM((quarter, pixels), low),
            sem((height_size,)),
            *[pltpu.VMEM((pixels, SCORE_ROWS), wide)] * (pixels // SCORE_ROWS),
        ],
        [held_proj, normed, query, key, value, soft, out_flip, *grad_pieces],
        "vvvvvvvh" + "a" * (height_size - 1),
        3 * dot_flops + 4 * score_flops,
        20,
    )
    mixed = trade_canvas(mixed)
    halves = [((18 * out_share, ci_share), low)] * 2
    residual_grad, grad_two, sums, keep_two, send_two = call_kernel(
        functools.partial(third_kernel, cols=cols),
        [plane_wide, plane, sums_shape, *halves],
        [held_wide, narrow, columns, part_held],
        [held_qkv, all_grad, packed, residual, table, act_two, lane_mask, sums],
        "vvvvvvvv",
        3 * dot_flops + conv_flops // height_size,
        16,
    )
    grad_two, *mixed = lax.optimization_barrier((grad_two, *mixed))
    mixed_sum = mixed[0].astype(wide)
    for piece in mixed[1:]:
        mixed_sum = mixed_sum + piece.astype(wide)
    joints = trade_canvas([mixed_sum.astype(low)] * canvas_size)
    act_two_grad, partial_sums = call_kernel(
        functools.partial(turn_kernel, cols=cols),
        [plane_wide, sums_shape],
        [taps],
        [grad_two, mask, turned, middle, table],
        "vvvvv",
        conv_flops,
        16,
    )
    act_two_grad, *joints = lax.optimization_barrier((act_two_grad, *joints))
    (own_mixed,) = call_kernel(
        place_kernel,
        [((quarter, 4 * channels), low)],
        [],
        joints,
        "v" * canvas_size,
        1,
        12,
    )
    own_mixed, send_two = lax.optimization_barrier((own_mixed, send_two))
    got_two = send_canvas(send_two, 2)
    chip_mixed = send_height(own_mixed, 2)
    core_mixed = send_height(own_mixed, 1)
    grad_one, sums, keep_one, send_one = call_kernel(
        functools.partial(second_kernel, cols=cols),
        [plane, sums_shape, *halves],
        [narrow, columns, part_held, pltpu.VMEM((8, channels), wide)],
        [act_two_grad, partial_sums, middle, table, act_one, lane_mask, sums],
        "vvvvvvv",
        1,
        16,
    )
    got_one = send_canvas(send_one, 1)

    own_total, sums, partial_sums = call_kernel(
        functools.partial(first_kernel, cols=cols),
        [((own_pixels, channels), wide), sums_shape, sums_shape],
        [held_wide, taps],
        [grad_one, all_features, table, mask, sums, turned],
        "vvvvvv",
        1,
        20,
    )
    (input_grad,) = call_kernel(
        own_kernel,
        [((own_pixels, channels), low)],
        [],
        [own_total, partial_sums, all_features, residual_grad, table],
        "vvvvv",
        dot_flops // 4,
        12,
        "o",
    )
    input_grad, sums, core_mixed, got_one, got_two = lax.optimization_barrier(
        (input_grad, sums, core_mixed, got_one, got_two)
    )
    share_rows = 9 * out_share
    send_rows = share_rows + sums_shape[0][0] * channels // LANES
    hold_one, send_one, hold_two, send_two = call_kernel(
        halve_sums_kernel,
        [((share_rows, ci_share), wide), ((send_rows, ci_share), low)] * 2,
        [],
        [keep_one, got_one, keep_two, got_two, sums],
        "vvvvv",
        1,
        12,
    )
    got_two = send_canvas(send_two, 1)
    got_one = send_canvas(send_one, 2)
    far_sums = send_canvas(sums, 3)
    chip_mixed, hold_one = lax.optimization_barrier((chip_mixed, hold_one))
    both_mixed = send_height(chip_mixed, 1)
    qkv_grad, proj_grad = call_kernel(
        join_kernel,
        [(qkv_weight.shape, wide), (proj_weight.shape, wide)],
        [
            pltpu.VMEM((4, quarter, 3 * channels), wide),
            pltpu.VMEM((4, quarter, channels), wide),
            sem((4, 2)),
        ],
        [own_mixed, chip_mixed, core_mixed, both_mixed],
        "vvvv",
        conv_flops,
        12,
        "hh",
    )
    qkv_grad, got_one, got_two, far_sums = lax.optimization_barrier(
        (qkv_grad, got_one, got_two, far_sums)
    )
    vector_shapes = [norm_gains.shape, norm_shifts.shape, conv_biases.shape, qv_bias.shape]
    conv_grad, gains_grad, shifts_grad, biases_grad, qv_grad, proj_bias_grad = call_kernel(
        sums_kernel,
        [((2, 3, 3, out_share, ci_share), wide)]
        + [(shape, wide) for shape in vector_shapes + [(1, channels)]],
        [],
        [sums, far_sums, hold_one, got_one, hold_two, got_two],
        "vvvvvv",
        1,
        12,
        "o" * 6,
    )
    own_shape = (1, local_rows, cols, channels)
    return (
        output.reshape(own_shape),
        input_grad.reshape(own_shape),
        gains_grad,
        shifts_grad,
        jnp.swapaxes(conv_grad, 3, 4),
        biases_grad,
        qkv_grad,
        qv_grad,
        proj_grad,
        proj_bias_grad.reshape(channels),
    )


def on_device(*arrays):
    features, tile_ids = arrays[0], arrays[1]
    local_rows, cols, channels = features.shape[1:]
    pixels = tile_ids.shape[1] * cols
    height_size, canvas_size = lax.axis_size("height"), lax.axis_size("canvas")
    powers = all(size & (size - 1) == 0 for size in (height_size, canvas_size, cols))
    fits = (
        powers
        and height_size > 2
        and canvas_size == 4
        and channels == LANES * canvas_size
        and pixels <= MOST_PIXELS
        and pixels % FILL_ROWS == 0
        and FILL_ROWS % CHUNK == 0
        and pixels % SCORE_ROWS == 0
        and pixels % KEY_ROWS == 0
        and (local_rows * cols) % LANES == 0
        and CHUNK % cols == 0
        and cols % 16 == 0
        and channels % (LANES * canvas_size) == 0
        and 2 * channels == NARROW * height_size
    )
    return whole_canvas(*arrays) if fits else split_canvas(*arrays)


def solution(mesh):
    in_specs = (
        P("canvas", "height", None, None),
        P("canvas", None),
        P(),
        P(),
        P(),
        P(),
        P(),
        P(),
        P(),
        P(),
        P("canvas", "height", None, None),
    )
    out_specs = (
        P("canvas", "height", None, None),
        P("canvas", "height", None, None),
        P(),
        P(),
        P(None, None, None, "canvas", "height"),
        P(),
        P(),
        P(),
        P(),
        P(),
    )
    return jax.shard_map(
        on_device, mesh=mesh, in_specs=in_specs, out_specs=out_specs, check_vma=False
    )
```

```python
import functools

import jax
import jax.numpy as jnp
from jax import lax
from jax.experimental import pallas as pl
from jax.experimental.pallas import tpu as pltpu
from jax.sharding import PartitionSpec as P

GROUPS = 32


epsilon = 1e-06
masked_score = -1e30
MOST_PIXELS = 1024
LANES = 128
NARROW = 128
CHUNK = 128
FILL_ROWS = 256
QUERY_ROWS = 512
SCORE_ROWS = 256
KEY_ROWS = 256


def extended(block, sides, width):
    for axis, dim in sides:
        count = lax.axis_size(axis)
        forward = [(i, i + 1) for i in range(count - 1)]
        backward = [(target, source) for source, target in forward]
        low = lax.ppermute(
            lax.slice_in_dim(block, block.shape[dim] - width, None, axis=dim), axis, forward
        )
        high = lax.ppermute(lax.slice_in_dim(block, 0, width, axis=dim), axis, backward)
        block = jnp.concatenate([low, block, high], axis=dim)
    return block


def group_total(vector):
    return vector.reshape(GROUPS, -1).sum(axis=1)


def spread_groups(vector, channels):
    return jnp.repeat(vector, channels // GROUPS)


def norm_forward(values, gain, shift, members):
    channels = values.shape[1]
    totals = lax.psum(group_total(jnp.sum(values, axis=0)), "height")
    centered = values - spread_groups(totals / members, channels)
    squares = lax.psum(group_total(jnp.sum(centered * centered, axis=0)), "height")
    inverse = spread_groups(lax.rsqrt(squares / members + epsilon), channels)
    normed = centered * inverse
    return (normed, inverse, normed * gain + shift)


def norm_backward(grad_in, normed, inverse, gain, members):
    channels = grad_in.shape[1]
    scaled = grad_in * gain
    both_sums = lax.psum(
        (group_total(jnp.sum(scaled, axis=0)), group_total(jnp.sum(scaled * normed, axis=0))),
        "height",
    )
    mean_grad = spread_groups(both_sums[0] / members, channels)
    mean_cross = spread_groups(both_sums[1] / members, channels)
    result = inverse * (scaled - mean_grad - normed * mean_cross)
    return (result, jnp.sum(grad_in * normed, axis=0), jnp.sum(grad_in, axis=0))


def swish(values):
    return values * jax.nn.sigmoid(values)


def swish_slope(values):
    sigmoid_part = jax.nn.sigmoid(values)
    return sigmoid_part * (1.0 + values * (1.0 - sigmoid_part))


def tap_columns(padded, row_mask, local_rows, canvas_cols):
    pieces = []
    for row_tap in range(3):
        rows_taken = padded[row_tap : row_tap + local_rows] * row_mask[:, row_tap, None, None]
        for col_tap in range(3):
            pieces.append(rows_taken[:, col_tap : col_tap + canvas_cols])
    stacked = jnp.concatenate(pieces, axis=2)
    return stacked.reshape(local_rows * canvas_cols, stacked.shape[2])


def conv_forward(acts, row_mask, weight, bias):
    local_rows, canvas_cols, channels = acts.shape
    rimmed = extended(acts, (("height", 0),), 1)
    padded = jnp.pad(rimmed, ((0, 0), (1, 1), (0, 0)))
    gathered = tap_columns(padded, row_mask, local_rows, canvas_cols)
    result = (
        jnp.dot(
            gathered, weight.reshape(9 * channels, channels), preferred_element_type=jnp.float32
        )
        + bias
    )
    return (result, gathered)


def conv_backward(grad_low, row_mask, weight, gathered):
    local_rows, canvas_cols, channels = grad_low.shape
    flat_grad = grad_low.reshape(local_rows * canvas_cols, channels)
    weight_grad = lax.dot_general(
        gathered, flat_grad, (((0,), (0,)), ((), ())), preferred_element_type=jnp.float32
    )
    rimmed = extended(grad_low, (("height", 0),), 1)
    padded = jnp.pad(rimmed, ((0, 0), (1, 1), (0, 0)))
    grad_taps = tap_columns(padded, row_mask, local_rows, canvas_cols)
    flipped = jnp.transpose(weight[::-1, ::-1], (0, 1, 3, 2)).reshape(9 * channels, channels)
    input_part = jnp.dot(grad_taps, flipped, preferred_element_type=jnp.float32)
    return (
        input_part,
        weight_grad.reshape(3, 3, channels, channels),
        jnp.sum(flat_grad.astype(jnp.float32), axis=0),
    )


def take_rows(array, offset, count):
    return lax.dynamic_slice_in_dim(array, offset, count)


def score_grads(
    queries, out_grad, log_total, row_dots, query_ids, key_rows, value_rows, key_ids, score_scale
):
    scores = (
        lax.dot_general(
            queries, key_rows, (((1,), (1,)), ((), ())), preferred_element_type=jnp.float32
        )
        * score_scale
    )
    same_tile = query_ids[:, None] == key_ids[None, :]
    softmax_block = jnp.exp(jnp.where(same_tile, scores - log_total[:, None], masked_score))
    weight_grad = lax.dot_general(
        out_grad, value_rows, (((1,), (1,)), ((), ())), preferred_element_type=jnp.float32
    )
    score_grad = (softmax_block * (weight_grad - row_dots[:, None])).astype(jnp.bfloat16)
    return (softmax_block.astype(jnp.bfloat16), score_grad)


def split_canvas(
    features,
    tile_ids,
    norm_gains,
    norm_shifts,
    conv_weights,
    conv_biases,
    qkv_weight,
    qv_bias,
    proj_weight,
    proj_bias,
    cotangent,
):
    height_size = lax.axis_size("height")
    local_rows = features.shape[1]
    canvas_cols = features.shape[2]
    channels = features.shape[3]
    pixels = local_rows * canvas_cols
    row_ids = tile_ids[0]
    all_rows = row_ids.shape[0]
    members = float(all_rows * canvas_cols * (channels // GROUPS))
    score_scale = channels ** (-0.5)
    first_row = lax.axis_index("height") * local_rows
    edge_ids = jnp.full((1,), -1, jnp.int32)
    padded_ids = jnp.concatenate([edge_ids, row_ids, edge_ids])
    near_ids = lax.dynamic_slice_in_dim(padded_ids, first_row, local_rows + 2)
    own_rows = near_ids[1 : local_rows + 1]
    row_mask = jnp.stack(
        [near_ids[row_tap : row_tap + local_rows] == own_rows for row_tap in range(3)], axis=1
    ).astype(jnp.bfloat16)
    key_ids = jnp.repeat(row_ids, canvas_cols)
    query_ids = jnp.repeat(own_rows, canvas_cols)
    grid_shape = (local_rows, canvas_cols, channels)
    inputs = features[0].reshape(pixels, channels).astype(jnp.float32)
    normed_one, inverse_one, pre_one = norm_forward(inputs, norm_gains[0], norm_shifts[0], members)
    act_one = swish(pre_one).astype(jnp.bfloat16).reshape(grid_shape)
    middle, taps_one = conv_forward(act_one, row_mask, conv_weights[0], conv_biases[0])
    normed_two, inverse_two, pre_two = norm_forward(middle, norm_gains[1], norm_shifts[1], members)
    act_two = swish(pre_two).astype(jnp.bfloat16).reshape(grid_shape)
    branch, taps_two = conv_forward(act_two, row_mask, conv_weights[1], conv_biases[1])
    residual = inputs + branch
    normed_three, inverse_three, pre_three = norm_forward(
        residual, norm_gains[2], norm_shifts[2], members
    )
    attn_input = pre_three.astype(jnp.bfloat16)
    mixed = jnp.dot(attn_input, qkv_weight, preferred_element_type=jnp.float32)
    queries = (mixed[:, :channels] + qv_bias[0]).astype(jnp.bfloat16)
    key_rows = mixed[:, channels : 2 * channels].astype(jnp.bfloat16)
    value_rows = (mixed[:, 2 * channels :] + qv_bias[1]).astype(jnp.bfloat16)
    running_max = jnp.full((pixels,), masked_score, jnp.float32)
    key_piece = lax.all_gather(key_rows, "height", axis=0, tiled=True)
    value_piece = lax.all_gather(value_rows, "height", axis=0, tiled=True)
    scores = (
        lax.dot_general(
            queries, key_piece, (((1,), (1,)), ((), ())), preferred_element_type=jnp.float32
        )
        * score_scale
    )
    same_tile = query_ids[:, None] == key_ids[None, :]
    scores = jnp.where(same_tile, scores, masked_score)
    new_max = jnp.maximum(running_max, jnp.max(scores, axis=1))
    weights = jnp.where(same_tile, jnp.exp(scores - new_max[:, None]), 0.0)
    summed_out = jnp.dot(
        weights.astype(jnp.bfloat16), value_piece, preferred_element_type=jnp.float32
    )
    total_weight = jnp.sum(weights, axis=1)
    log_total = new_max + jnp.log(total_weight)
    attended = summed_out / total_weight[:, None]
    attended_low = attended.astype(jnp.bfloat16)
    output = (
        residual
        + jnp.dot(attended_low, proj_weight, preferred_element_type=jnp.float32)
        + proj_bias
    )
    out_grad = cotangent[0].reshape(pixels, channels)
    out_grad_full = out_grad.astype(jnp.float32)
    proj_grad = lax.dot_general(
        attended_low, out_grad, (((0,), (0,)), ((), ())), preferred_element_type=jnp.float32
    )
    proj_bias_grad = jnp.sum(out_grad_full, axis=0)
    attended_grad = lax.dot_general(
        out_grad, proj_weight, (((1,), (1,)), ((), ())), preferred_element_type=jnp.float32
    ).astype(jnp.bfloat16)
    row_dots = jnp.sum(attended_grad.astype(jnp.float32) * attended, axis=1)
    block_rows = pixels * min(height_size, 8)
    zero_block = jnp.zeros((pixels, channels), jnp.float32)
    key_all, value_all = (
        lax.all_gather(key_rows, "height", axis=0, tiled=True),
        lax.all_gather(value_rows, "height", axis=0, tiled=True),
    )
    query_all, grad_all = (
        lax.all_gather(queries, "height", axis=0, tiled=True),
        lax.all_gather(attended_grad, "height", axis=0, tiled=True),
    )
    total_all, dots_all = (
        lax.all_gather(log_total, "height", axis=0, tiled=True),
        lax.all_gather(row_dots, "height", axis=0, tiled=True),
    )

    def own_query_step(running, block_index):
        offset = block_index * block_rows
        key_part = take_rows(key_all, offset, block_rows)
        rounded, score_grad = score_grads(
            queries,
            attended_grad,
            log_total,
            row_dots,
            query_ids,
            key_part,
            take_rows(value_all, offset, block_rows),
            take_rows(key_ids, offset, block_rows),
            score_scale,
        )
        return (
            running
            + jnp.dot(score_grad, key_part, preferred_element_type=jnp.float32) * score_scale,
            None,
        )

    def own_key_step(running, block_index):
        offset = block_index * block_rows
        query_part = take_rows(query_all, offset, block_rows)
        grad_part = take_rows(grad_all, offset, block_rows)
        rounded, score_grad = score_grads(
            query_part,
            grad_part,
            take_rows(total_all, offset, block_rows),
            take_rows(dots_all, offset, block_rows),
            take_rows(key_ids, offset, block_rows),
            key_rows,
            value_rows,
            query_ids,
            score_scale,
        )
        key_part = (
            lax.dot_general(
                score_grad, query_part, (((0,), (0,)), ((), ())), preferred_element_type=jnp.float32
            )
            * score_scale
        )
        value_part = lax.dot_general(
            rounded, grad_part, (((0,), (0,)), ((), ())), preferred_element_type=jnp.float32
        )
        return ((running[0] + key_part, running[1] + value_part), None)

    block_count = key_all.shape[0] // block_rows
    query_grad, unused_one = lax.scan(own_query_step, zero_block, jnp.arange(block_count))
    (key_grad, value_grad), unused_two = lax.scan(
        own_key_step, (zero_block, zero_block), jnp.arange(block_count)
    )
    query_low = query_grad.astype(jnp.bfloat16)
    key_low = key_grad.astype(jnp.bfloat16)
    value_low = value_grad.astype(jnp.bfloat16)
    stacked_grad = jnp.concatenate([query_low, key_low, value_low], axis=1)
    qkv_grad = lax.dot_general(
        attn_input, stacked_grad, (((0,), (0,)), ((), ())), preferred_element_type=jnp.float32
    )
    qv_grad = jnp.stack(
        [
            jnp.sum(query_low.astype(jnp.float32), axis=0),
            jnp.sum(value_low.astype(jnp.float32), axis=0),
        ]
    )
    normed_grad = lax.dot_general(
        stacked_grad, qkv_weight, (((1,), (1,)), ((), ())), preferred_element_type=jnp.float32
    )
    back_three, gain_three, shift_three = norm_backward(
        normed_grad, normed_three, inverse_three, norm_gains[2], members
    )
    residual_grad = out_grad_full + back_three
    grad_two = residual_grad.astype(jnp.bfloat16).reshape(grid_shape)
    act_two_grad, weight_two_grad, bias_two_grad = conv_backward(
        grad_two, row_mask, conv_weights[1], taps_two
    )
    middle_grad, gain_two, shift_two = norm_backward(
        act_two_grad * swish_slope(pre_two), normed_two, inverse_two, norm_gains[1], members
    )
    grad_one = middle_grad.astype(jnp.bfloat16).reshape(grid_shape)
    act_one_grad, weight_one_grad, bias_one_grad = conv_backward(
        grad_one, row_mask, conv_weights[0], taps_one
    )
    input_back, gain_one, shift_one = norm_backward(
        act_one_grad * swish_slope(pre_one), normed_one, inverse_one, norm_gains[0], members
    )
    input_grad = residual_grad + input_back
    conv_grad = jnp.stack([weight_one_grad, weight_two_grad])
    conv_part = lax.psum_scatter(conv_grad, "height", scatter_dimension=4, tiled=True)
    conv_part = lax.psum_scatter(
        conv_part.astype(jnp.bfloat16), "canvas", scatter_dimension=3, tiled=True
    ).astype(jnp.float32)
    summed = lax.psum(
        (
            jnp.stack([gain_one, gain_two, gain_three]),
            jnp.stack([shift_one, shift_two, shift_three]),
            jnp.stack([bias_one_grad, bias_two_grad]),
            qkv_grad,
            qv_grad,
            proj_grad,
            proj_bias_grad,
        ),
        ("canvas", "height"),
    )
    return (
        output.astype(jnp.bfloat16).reshape((1,) + grid_shape),
        input_grad.astype(jnp.bfloat16).reshape((1,) + grid_shape),
        summed[0],
        summed[1],
        conv_part,
        summed[2],
        summed[3],
        summed[4],
        summed[5],
        summed[6],
    )


def fold(block):
    rows, width = block.shape
    return jnp.sum(block.reshape(rows // 8, 8, width), axis=0)


def group_lanes(block, group):
    lane = lax.broadcasted_iota(jnp.int32, block.shape, 1)
    width = block.shape[1]
    step = 1
    while step < group:
        above = pltpu.roll(block, step, 1)
        below = pltpu.roll(block, width - step, 1)
        block = block + jnp.where((lane & step) != 0, above, below)
        step *= 2
    return block


def group_mean(partial, members):
    spread = group_lanes(partial, partial.shape[1] // GROUPS)
    return jnp.sum(spread, axis=0, keepdims=True) * (1.0 / members)


def widen(block, width):
    return jnp.concatenate([block] * (width // block.shape[1]), axis=1)


def each_block(pixels, block, body, carry=0):
    def step(index, carry):
        return body(pl.ds(pl.multiple_of(index * block, block), block), carry)

    return lax.fori_loop(0, pixels // block, step, carry)


def each_chunk(pixels, body, carry):
    return each_block(pixels, CHUNK, body, carry)


def aligned(start, step):
    return start if isinstance(start, int) else pl.multiple_of(start, step)


class RunningStats:
    def __init__(self, channels):
        self.width = channels // GROUPS
        self.reference = None
        self.sums = self.squares = jnp.zeros((8, channels), jnp.float32)

    def add(self, block):
        if self.reference is None:
            self.reference = group_mean(block[0:8], 8.0 * self.width)
        offset = block - self.reference
        self.sums = self.sums + fold(offset)
        self.squares = self.squares + fold(offset * offset)

    def finish(self, pixels):
        both = group_lanes(jnp.concatenate([self.sums, self.squares], axis=0), self.width)
        share = 1.0 / (pixels * self.width)
        offset = column_total(both[0:8]) * share
        variance = column_total(both[8:16]) * share - offset * offset
        return self.reference + offset, lax.rsqrt(jnp.maximum(variance, 0.0) + epsilon)


def put_taps(taps_ref, block, rows, cols):
    count, channels = block.shape
    place = lax.broadcasted_iota(jnp.int32, block.shape, 0) & (cols - 1)
    left = jnp.where(place == 0, 0.0, pltpu.roll(block, 1, 0))
    right = jnp.where(place == cols - 1, 0.0, pltpu.roll(block, count - 1, 0))
    inner = pl.ds(aligned(rows.start + cols, cols), count)
    taps_ref[inner, 0:channels] = left.astype(jnp.bfloat16)
    taps_ref[inner, channels : 2 * channels] = block.astype(jnp.bfloat16)
    taps_ref[inner, 2 * channels :] = right.astype(jnp.bfloat16)


def clear_edges(taps_ref, cols):
    edge = jnp.zeros((cols, taps_ref.shape[1]), taps_ref.dtype)
    taps_ref[0:cols, :] = edge
    taps_ref[taps_ref.shape[0] - cols :, :] = edge


def begin_conv(taps_ref, product, total_ref, fill, first, cols):
    for start in range(0, total_ref.shape[0], FILL_ROWS):
        for inner in range(start, start + FILL_ROWS, CHUNK):
            fill(pl.ds(inner, CHUNK))
        rows = pl.ds(start, FILL_ROWS)
        total_ref[rows, :] = first(rows, product(taps_ref, pl.ds(start + cols, FILL_ROWS), 1))


def add_rows(taps_ref, product, mask_ref, total_ref, row_tap, last, cols, old_ref=None):
    pixels, channels = total_ref.shape
    old_ref = total_ref if old_ref is None else old_ref

    def step(rows, shifted):
        part = product(taps_ref, shifted, row_tap)
        mask = widen(mask_ref[row_tap // 2, rows, :], channels)
        value = old_ref[rows, :] + mask * part
        total_ref[rows, :] = value if last is None else last(rows, value)

    block = 2 * FILL_ROWS if last is None else FILL_ROWS
    for start in range(0, pixels, block):
        step(pl.ds(start, block), pl.ds(start + row_tap * cols, block))


def run_conv(taps_ref, product, mask_ref, total_ref, fill, first, last, cols):
    begin_conv(taps_ref, product, total_ref, fill, first, cols)
    add_rows(taps_ref, product, mask_ref, total_ref, 0, None, cols)
    add_rows(taps_ref, product, mask_ref, total_ref, 2, last, cols)


def product_forward(weight_ref):
    channels = weight_ref.shape[-1]

    def product(taps_ref, shifted, row_tap):
        return jnp.dot(
            taps_ref[shifted, :],
            weight_ref[row_tap].reshape(3 * channels, channels),
            preferred_element_type=jnp.float32,
        )

    return product


def product_backward(weight_ref):
    def product(taps_ref, shifted, row_tap):
        return lax.dot_general(
            taps_ref[shifted, :],
            weight_ref[row_tap],
            (((1,), (1,)), ((), ())),
            preferred_element_type=jnp.float32,
        )

    return product


def activation(read, mean, inverse, gain, shift, act_ref, taps_ref, cols):
    scale, offset = 0.5 * inverse * gain, 0.5 * shift

    def fill(rows):
        half = (read(rows) - mean) * scale + offset
        act = half * (1.0 + jnp.tanh(half))
        act_ref[rows, :] = act.astype(jnp.bfloat16)
        put_taps(taps_ref, act, rows, cols)

    return fill


def back_means(sums, gain, pixels):
    channels = gain.shape[1]
    members = float(pixels * (channels // GROUPS))
    return group_mean(sums[0] * gain, members), group_mean(sums[1] * gain, members)


def column_total(partial):
    return jnp.sum(partial, axis=0, keepdims=True)


def weight_part(act_ref, narrow, lanes_ref, flip_ref, columns_ref, part_ref, cols):
    pixels, channels = act_ref.shape
    height = lax.axis_index("height")
    share = NARROW // 2
    flip_ref[...] = narrow.T
    own = pl.ds(pl.multiple_of((height % 2) * share, share), share)
    grad = flip_ref[own, :].astype(jnp.float32)
    column = lax.broadcasted_iota(jnp.int32, grad.shape, 1) & (cols - 1)
    for col_tap in range(3):
        shifted = grad
        if col_tap == 0:
            shifted = jnp.where(column == cols - 1, 0.0, pltpu.roll(grad, pixels - 1, 1))
        elif col_tap == 2:
            shifted = jnp.where(column == 0, 0.0, pltpu.roll(grad, 1, 1))
        for row_tap in range(3):
            tap = 3 * row_tap + col_tap
            place = slice(tap * share, (tap + 1) * share)
            if row_tap == 1:
                columns_ref[place, :] = shifted.astype(jnp.bfloat16)
                continue
            side, turn = (0, pixels - cols) if row_tap == 0 else (1, cols)
            masked = (shifted * lanes_ref[side : side + 1, :]).astype(jnp.bfloat16)
            columns_ref[place, :] = pltpu.roll(masked, turn, 1)
    part_ref[...] = jnp.dot(
        columns_ref[...], act_ref[...], preferred_element_type=jnp.float32
    ).astype(jnp.bfloat16)


def begin_back(grad_ref, weights_ref, mask_ref, taps_ref, total_ref, cols):
    clear_edges(taps_ref, cols)

    def fill(rows):
        put_taps(taps_ref, grad_ref[rows, :].astype(jnp.float32), rows, cols)

    product = product_backward(weights_ref)
    begin_conv(taps_ref, product, total_ref, fill, lambda rows, part: part, cols)
    add_rows(taps_ref, product, mask_ref, total_ref, 0, None, cols)


def finish_back(
    weights_ref, mask_ref, taps_ref, total_ref, read, table_ref, which, cols, old_ref=None
):
    mean, inverse, gain, shift = norm_rows(table_ref, which)
    scale, offset = 0.5 * inverse * gain, 0.5 * shift
    sums = []

    def slope(rows, value):
        centered = read(rows) - mean
        half = centered * scale + offset
        turn = jnp.tanh(half)
        double = value * ((1.0 + turn) * (1.0 + half * (1.0 - turn)))
        sums.append((fold(double), fold(double * centered)))
        return double

    add_rows(
        taps_ref, product_backward(weights_ref), mask_ref, total_ref, 2, slope, cols, old_ref
    )
    plain, cross = sum(pair[0] for pair in sums), sum(pair[1] for pair in sums)
    return 0.5 * plain, 0.5 * inverse * cross


def norm_back(total_ref, double, sums, read, table_ref, which, pixels, scales_ref=None):
    mean, inverse, gain, shift = norm_rows(table_ref, which)
    mean_grad, mean_cross = back_means(sums, gain, pixels)
    slope = inverse * gain * (0.5 if double else 1.0)
    level, tilt = inverse * mean_grad, inverse * inverse * mean_cross
    if scales_ref is not None:
        for row, scales in enumerate((mean, slope, level, tilt)):
            scales_ref[row : row + 1, :] = scales

    def back(rows, inner):
        return total_ref[inner, :] * slope - level - (read(rows) - mean) * tilt

    return back


def own_lanes():
    block = lax.axis_index("height") // 2
    return pl.ds(pl.multiple_of(block * NARROW, NARROW), NARROW)


def narrow_back(total_ref, value_ref, scales_ref):
    lanes = own_lanes()
    mean, slope, level, tilt = (scales_ref[row : row + 1, lanes] for row in range(4))
    return total_ref[:, lanes] * slope - level - (value_ref[:, lanes] - mean) * tilt


def turn_kernel(grad_ref, mask_ref, weights_ref, total_ref, taps_ref, *, cols):
    begin_back(grad_ref, weights_ref.at[1], mask_ref, taps_ref, total_ref, cols)


def norm_rows(table_ref, which):
    picks = (2 * which, 2 * which + 1, 6 + which, 9 + which)
    return tuple(table_ref[pick : pick + 1, :] for pick in picks)


def build_masks(ids_ref, mask_ref, lanes_ref, id_rows_ref, id_cols_ref, cols):
    rows = ids_ref.shape[1]

    def one_row(row, carry):
        here = ids_ref[0, row]
        place = pl.ds(pl.multiple_of(row * cols, cols), cols)
        id_rows_ref[place, :] = jnp.full((cols, LANES), here, jnp.int32)
        for side, other in ((0, row - 1), (1, row + 1)):
            inside = jnp.logical_and(other >= 0, other < rows)
            other_id = ids_ref[0, jnp.clip(other, 0, rows - 1)]
            same = jnp.where(jnp.logical_and(inside, other_id == here), 1.0, 0.0)
            mask_ref[side, place, :] = jnp.full((cols, LANES), same, jnp.float32)
        return carry

    lax.fori_loop(0, rows, one_row, 0)
    lane = lax.broadcasted_iota(jnp.int32, (8, LANES), 1)
    each = LANES // cols
    for block in range(rows // each):
        ids = jnp.full((8, LANES), ids_ref[0, block * each], jnp.int32)
        for step in range(1, each):
            ids = jnp.where(lane >= step * cols, ids_ref[0, block * each + step], ids)
        id_cols_ref[:, block * LANES : (block + 1) * LANES] = ids
    ids = id_cols_ref[...].astype(jnp.float32)
    pixels = ids.shape[1]
    pixel = lax.broadcasted_iota(jnp.int32, ids.shape, 1)
    above = jnp.where(pixel < cols, -1.0, pltpu.roll(ids, cols, 1))
    below = jnp.where(pixel >= pixels - cols, -1.0, pltpu.roll(ids, pixels - cols, 1))
    lanes_ref[0:1, :] = jnp.where(above == ids, 1.0, 0.0)[0:1]
    lanes_ref[1:2, :] = jnp.where(below == ids, 1.0, 0.0)[0:1]


def place_pieces(pieces, whole_ref, sems):
    own_pixels = whole_ref.shape[0] // len(pieces)
    height = lax.axis_index("height")
    copies = []
    for place, piece in enumerate(pieces):
        start = pl.multiple_of((height ^ place) * own_pixels, own_pixels)
        rows = pl.ds(start, own_pixels)
        copies.append(pltpu.make_async_copy(piece, whole_ref.at[rows, :], sems.at[place]))
    return copies


def hold_kernel(
    ids_hbm,
    gains_hbm,
    shifts_hbm,
    biases_hbm,
    weights_hbm,
    qkv_hbm,
    proj_hbm,
    qv_bias_hbm,
    proj_bias_hbm,
    weights_ref,
    turned_ref,
    qkv_ref,
    proj_ref,
    table_ref,
    mask_ref,
    lanes_ref,
    id_rows_ref,
    id_cols_ref,
    ids_ref,
    gains_ref,
    shifts_ref,
    biases_ref,
    qv_bias_ref,
    proj_bias_ref,
    sems,
    *,
    cols,
):
    channels = weights_ref.shape[-1]
    small = [
        (ids_hbm, ids_ref),
        (gains_hbm, gains_ref),
        (shifts_hbm, shifts_ref),
        (biases_hbm, biases_ref),
        (qv_bias_hbm, qv_bias_ref),
        (proj_bias_hbm, proj_bias_ref),
    ]
    large = [(weights_hbm, weights_ref), (qkv_hbm, qkv_ref), (proj_hbm, proj_ref)]
    for which in range(2):
        for row_tap in range(3):
            for col_tap in range(3):
                place = slice(col_tap * channels, (col_tap + 1) * channels)
                large.append(
                    (
                        weights_hbm.at[which, 2 - row_tap, 2 - col_tap],
                        turned_ref.at[which, row_tap, :, place],
                    )
                )
    copies = [
        pltpu.make_async_copy(source, target, sems.at[index])
        for index, (source, target) in enumerate(small + large)
    ]
    for copy in copies:
        copy.start()
    for copy in copies[: len(small)]:
        copy.wait()
    build_masks(ids_ref, mask_ref, lanes_ref, id_rows_ref, id_cols_ref, cols)
    table_ref[6:9, :] = gains_ref[...]
    table_ref[9:12, :] = shifts_ref[...]
    table_ref[12:14, :] = biases_ref[...]
    table_ref[14:16, :] = qv_bias_ref[...]
    table_ref[16:17, :] = proj_bias_ref[...]
    for copy in copies[len(small) :]:
        copy.wait()


def conv_kernel(*refs, cols, count):
    pieces, refs = refs[:count], refs[count:]
    (
        weights_ref,
        params_ref,
        mask_ref,
        features_ref,
        act_one_ref,
        middle_ref,
        act_two_ref,
        residual_ref,
        table_ref,
        own_ref,
        taps_ref,
        sem,
    ) = refs
    pixels, channels = features_ref.shape
    wide = jnp.float32
    own_copy = pltpu.make_async_copy(pieces[0], own_ref, sem)
    own_copy.start()
    table_ref[...] = params_ref[...]
    clear_edges(taps_ref, cols)

    def read_input(rows):
        return features_ref[rows, :].astype(wide)

    def read_middle(rows):
        return middle_ref[rows, :]

    height = lax.axis_index("height")
    own_pixels = pixels // count
    seen = RunningStats(channels)
    for place in list(range(1, count)) + [0]:
        if place == 0:
            own_copy.wait()
        piece = (pieces[place] if place else own_ref)[...]
        start = pl.multiple_of((height ^ place) * own_pixels, own_pixels)
        features_ref[pl.ds(start, own_pixels), :] = piece
        seen.add(piece.astype(wide))
    table_ref[0:1, :], table_ref[1:2, :] = seen.finish(pixels)
    seen = RunningStats(channels)

    def keep(rows, value):
        seen.add(value)
        return value

    run_conv(
        taps_ref,
        product_forward(weights_ref.at[0]),
        mask_ref,
        middle_ref,
        activation(read_input, *norm_rows(table_ref, 0), act_one_ref, taps_ref, cols),
        lambda rows, part: part + table_ref[12:13, :],
        keep,
        cols,
    )
    table_ref[2:3, :], table_ref[3:4, :] = seen.finish(pixels)
    seen = RunningStats(channels)
    run_conv(
        taps_ref,
        product_forward(weights_ref.at[1]),
        mask_ref,
        residual_ref,
        activation(read_middle, *norm_rows(table_ref, 1), act_two_ref, taps_ref, cols),
        lambda rows, part: part + (read_input(rows) + table_ref[13:14, :]),
        keep,
        cols,
    )
    table_ref[4:5, :], table_ref[5:6, :] = seen.finish(pixels)


def score_kernel(
    qkv_ref,
    proj_ref,
    residual_ref,
    table_ref,
    id_rows_ref,
    id_cols_ref,
    normed_ref,
    query_ref,
    key_ref,
    value_ref,
    soft_ref,
    out_flip_ref,
    output_ref,
    value_flip_ref,
    *scores_refs,
    score_scale,
):
    pixels, channels = residual_ref.shape
    own_pixels = output_ref.shape[0]
    wide = jnp.float32
    exponent = score_scale * 1.4426950408889634
    mean, inverse, gain, shift = norm_rows(table_ref, 2)
    scale = inverse * gain

    def normalise(start):
        rows = slice(start, start + KEY_ROWS)
        normed = (residual_ref[rows, :] - mean) * scale + shift
        normed_ref[rows, :] = normed.astype(jnp.bfloat16)

    def project(start):
        rows = slice(start, start + KEY_ROWS)
        normed = normed_ref[rows, :]
        query_ref[rows, :] = (
            jnp.dot(normed, qkv_ref[:, 0:channels], preferred_element_type=wide)
            + table_ref[14:15, :]
        ).astype(jnp.bfloat16)
        key_ref[rows, :] = jnp.dot(
            normed, qkv_ref[:, channels : 2 * channels], preferred_element_type=wide
        ).astype(jnp.bfloat16)
        values = (
            jnp.dot(normed, qkv_ref[:, 2 * channels :], preferred_element_type=wide)
            + table_ref[15:16, :]
        ).astype(jnp.bfloat16)
        value_ref[rows, :] = values
        value_flip_ref[:, rows] = values.T

    normalise(0)
    for start in range(0, pixels, KEY_ROWS):
        if start + KEY_ROWS < pixels:
            normalise(start + KEY_ROWS)
        project(start)
    block = scores_refs[0].shape[1]
    steps = range(0, pixels, KEY_ROWS)

    def score(index):
        rows = slice(index * block, (index + 1) * block)
        for start in steps:
            keys = slice(start, start + KEY_ROWS)
            scores = lax.dot_general(
                key_ref[keys, :],
                query_ref[rows, :],
                (((1,), (1,)), ((), ())),
                preferred_element_type=wide,
            )
            same = widen(id_rows_ref[keys, :], block) == id_cols_ref[0:1, rows]
            scores_refs[index][keys, :] = jnp.where(same, scores, masked_score)

    def soften(index):
        rows = slice(index * block, (index + 1) * block)
        scores_ref = scores_refs[index]
        peak = jnp.full((8, block), masked_score, wide)
        for start in steps:
            scores = scores_ref[start : start + KEY_ROWS, :]
            peak = jnp.maximum(peak, jnp.max(scores.reshape(-1, 8, block), axis=0))
        peak = jnp.max(peak, axis=0, keepdims=True)
        total = jnp.zeros((8, block), wide)
        for start in steps:
            keys = slice(start, start + KEY_ROWS)
            powers = jnp.exp2((scores_ref[keys, :] - peak) * exponent)
            scores_ref[keys, :] = powers
            total = total + fold(powers)
        share = 1.0 / column_total(total)
        for start in steps:
            keys = slice(start, start + KEY_ROWS)
            soft_ref[keys, rows] = (scores_ref[keys, :] * share).astype(jnp.bfloat16)

    score(0)
    for index in range(len(scores_refs)):
        if index + 1 < len(scores_refs):
            score(index + 1)
        soften(index)

    def collect(rows, carry):
        out_flip_ref[rows, :] = jnp.dot(
            value_flip_ref[rows, :], soft_ref[...], preferred_element_type=wide
        ).astype(jnp.bfloat16)
        return carry

    each_block(channels, channels // 2, collect)
    height = lax.axis_index("height")
    own = pl.ds(pl.multiple_of(height * own_pixels, own_pixels), own_pixels)
    output_ref[...] = (
        residual_ref[own, :]
        + lax.dot_general(
            out_flip_ref[:, own],
            proj_ref[...],
            (((0,), (0,)), ((), ())),
            preferred_element_type=wide,
        )
        + table_ref[16:17, :]
    ).astype(jnp.bfloat16)


def own_quarter():
    height = lax.axis_index("height")
    return (height & 1) * 2 + ((height >> 1) & 1)


def attention_kernel(
    proj_ref,
    normed_ref,
    query_ref,
    key_ref,
    value_ref,
    soft_ref,
    out_flip_ref,
    *refs,
    score_scale,
    count,
):
    pieces, (grad_ref, packed_ref, sums_ref), refs = (
        refs[:count],
        refs[count : count + 3],
        refs[count + 3 :],
    )
    pixels, channels = normed_ref.shape
    blocks = pixels // SCORE_ROWS
    grads_refs, refs = refs[-blocks:], refs[:-blocks]
    keep_ref, send_ref, mixed_ref, key_flip_ref, back_ref, score_grad_ref, flip_ref, sems = refs
    wide = jnp.float32
    copies = place_pieces(pieces, grad_ref, sems)
    for copy in copies:
        copy.start()
    quarter = channels // 4
    own = pl.ds(pl.multiple_of(own_quarter() * quarter, quarter), quarter)
    flip_ref[...] = normed_ref[:, own].T
    key_flip_ref[...] = key_ref[...].T
    for copy in copies:
        copy.wait()
    block, count = SCORE_ROWS, blocks
    steps = range(0, pixels, KEY_ROWS)

    def block_rows(index):
        return slice(index * block, (index + 1) * block)

    for index in range(count):
        back_ref[block_rows(index), :] = lax.dot_general(
            grad_ref[block_rows(index), :],
            proj_ref[...],
            (((1,), (1,)), ((), ())),
            preferred_element_type=wide,
        ).astype(jnp.bfloat16)

    def weigh(index):
        total = jnp.zeros((8, block), wide)
        for start in steps:
            keys = slice(start, start + KEY_ROWS)
            weight_grad = lax.dot_general(
                value_ref[keys, :],
                back_ref[block_rows(index), :],
                (((1,), (1,)), ((), ())),
                preferred_element_type=wide,
            )
            grads_refs[index][keys, :] = weight_grad
            total = total + fold(soft_ref[keys, block_rows(index)].astype(wide) * weight_grad)
        return column_total(total)

    def slope(index, dots):
        for start in steps:
            keys = slice(start, start + KEY_ROWS)
            weights = soft_ref[keys, block_rows(index)].astype(wide)
            score_grad_ref[keys, block_rows(index)] = (
                weights * (grads_refs[index][keys, :] - dots)
            ).astype(jnp.bfloat16)

    dots = weigh(0)
    for index in range(count):
        now, rows = dots, block_rows(index)
        if index + 1 < count:
            dots = weigh(index + 1)
        slope(index, now)
        packed_ref[rows, 2 * channels :] = jnp.dot(
            soft_ref[rows, :], back_ref[...], preferred_element_type=wide
        ).astype(jnp.bfloat16)
        query_grad = jnp.dot(
            key_flip_ref[...], score_grad_ref[:, rows], preferred_element_type=wide
        )
        packed_ref[rows, 0:channels] = (query_grad * score_scale).astype(jnp.bfloat16).T
    for index in range(count):
        rows = block_rows(index)
        packed_ref[rows, channels : 2 * channels] = (
            jnp.dot(score_grad_ref[rows, :], query_ref[...], preferred_element_type=wide)
            * score_scale
        ).astype(jnp.bfloat16)

    def pack(rows, carry):
        return (
            carry[0] + fold(packed_ref[rows, 0:channels].astype(wide)),
            carry[1] + fold(packed_ref[rows, 2 * channels :].astype(wide)),
            carry[2] + fold(grad_ref[rows, :].astype(wide)),
        )

    zeros = jnp.zeros((8, channels), wide)
    totals = zeros, zeros, zeros
    for start in range(0, pixels, CHUNK):
        totals = pack(pl.ds(start, CHUNK), totals)
    sums_ref[...] = jnp.zeros(sums_ref.shape, wide)
    for row, total in enumerate(totals):
        sums_ref[8 + row : 9 + row, :] = column_total(total)
    mixed_ref[:, 0 : 3 * channels] = jnp.dot(
        flip_ref[...], packed_ref[...], preferred_element_type=wide
    ).astype(jnp.bfloat16)
    mixed_ref[:, 3 * channels :] = jnp.dot(
        out_flip_ref[own, :], grad_ref[...], preferred_element_type=wide
    ).astype(jnp.bfloat16)
    keep_half([mixed_ref], 0, keep_ref, send_ref)


def third_kernel(
    qkv_ref,
    grad_ref,
    packed_ref,
    residual_ref,
    table_ref,
    act_two_ref,
    lanes_ref,
    old_sums_ref,
    residual_grad_ref,
    grad_two_ref,
    sums_ref,
    part_ref,
    total_ref,
    flip_ref,
    columns_ref,
    *,
    cols,
):
    pixels, channels = residual_ref.shape
    block = FILL_ROWS
    wide = jnp.float32
    mean, inverse, gain, shift = norm_rows(table_ref, 2)
    zeros = jnp.zeros((8, channels), wide)

    sums = (zeros, zeros)
    for start in range(0, pixels, block):
        rows = pl.ds(start, block)
        normed_grad = lax.dot_general(
            packed_ref[rows, :], qkv_ref[...], (((1,), (1,)), ((), ())), preferred_element_type=wide
        )
        total_ref[rows, :] = normed_grad
        centered = residual_ref[rows, :] - mean
        sums = sums[0] + fold(normed_grad), sums[1] + fold(normed_grad * centered)
    sums = sums[0], sums[1] * inverse
    sums_ref[...] = old_sums_ref[...]
    sums_ref[5:6, :] = column_total(sums[1])
    sums_ref[6:7, :] = column_total(sums[0])
    back = norm_back(
        total_ref, False, sums, lambda rows: residual_ref[rows, :], table_ref, 2, pixels
    )

    def finish(rows, carry):
        total = grad_ref[rows, :].astype(wide) + back(rows, rows)
        residual_grad_ref[rows, :] = total
        low = total.astype(jnp.bfloat16)
        grad_two_ref[rows, :] = low
        return carry + fold(low.astype(wide))

    sums_ref[7:8, :] = column_total(each_chunk(pixels, finish, zeros))
    narrow = grad_two_ref[:, own_lanes()]
    weight_part(act_two_ref, narrow, lanes_ref, flip_ref, columns_ref, part_ref, cols)


def second_kernel(
    old_total_ref,
    taps_ref,
    middle_ref,
    table_ref,
    act_one_ref,
    mask_ref,
    lanes_ref,
    weights_ref,
    old_sums_ref,
    part_two_ref,
    grad_one_ref,
    sums_ref,
    keep_ref,
    send_ref,
    total_ref,
    flip_ref,
    columns_ref,
    part_ref,
    scales_ref,
    *,
    cols,
):
    pixels, channels = middle_ref.shape

    def read(rows):
        return middle_ref[rows, :]

    sums = finish_back(
        weights_ref.at[1], mask_ref, taps_ref, total_ref, read, table_ref, 1, cols, old_total_ref
    )
    back = norm_back(total_ref, True, sums, read, table_ref, 1, pixels, scales_ref)
    narrow = narrow_back(total_ref, middle_ref, scales_ref).astype(jnp.bfloat16)
    weight_part(act_one_ref, narrow, lanes_ref, flip_ref, columns_ref, part_ref, cols)
    sums_ref[...] = old_sums_ref[...]
    sums_ref[2:3, :] = column_total(sums[1])
    sums_ref[3:4, :] = column_total(sums[0])

    def finish(rows, carry):
        low = back(rows, rows).astype(jnp.bfloat16)
        grad_one_ref[rows, :] = low
        return carry + fold(low.astype(jnp.float32))

    zeros = jnp.zeros((8, channels), jnp.float32)
    sums_ref[4:5, :] = column_total(each_chunk(pixels, finish, zeros))
    keep_half([part_ref, part_two_ref], 1, keep_ref, send_ref)


def near_far():
    core = lax.axis_index("height") & 1
    return 1 + core, 2 - core


def keep_half(sources, axis, keep_ref, send_ref):
    me = lax.axis_index("canvas")
    near, far = near_far()
    for target_ref, flip in ((keep_ref, 0), (send_ref, near)):
        rows = target_ref.shape[0] // (2 * len(sources))
        start = 0
        for other in (0, far):
            owner = me ^ flip ^ other
            for source_ref in sources:
                target = target_ref.at[start : start + rows, :]
                if axis == 0:
                    place = pl.ds(pl.multiple_of(owner * rows, rows), rows)
                    target[...] = source_ref[place, :]
                else:
                    width = target_ref.shape[1]
                    place = pl.ds(pl.multiple_of(owner * width, width), width)
                    target[...] = source_ref[:, place]
                start += rows


def first_kernel(
    grad_one_ref,
    features_ref,
    table_ref,
    mask_ref,
    old_sums_ref,
    weights_ref,
    own_ref,
    sums_ref,
    partial_ref,
    total_ref,
    taps_ref,
    *,
    cols,
):
    def read(rows):
        return features_ref[rows, :].astype(jnp.float32)

    weights = weights_ref.at[0]
    begin_back(grad_one_ref, weights, mask_ref, taps_ref, total_ref, cols)
    sums = finish_back(weights, mask_ref, taps_ref, total_ref, read, table_ref, 0, cols)
    partial_ref[0:8, :], partial_ref[8:16, :] = sums
    sums_ref[...] = old_sums_ref[...]
    sums_ref[0:1, :] = column_total(sums[1])
    sums_ref[1:2, :] = column_total(sums[0])
    count = own_ref.shape[0]
    own = pl.ds(pl.multiple_of(lax.axis_index("height") * count, count), count)
    own_ref[...] = total_ref[own, :]


def own_kernel(
    own_ref, partial_ref, features_ref, residual_grad_ref, table_ref, input_grad_ref
):
    def read(rows):
        return features_ref[rows, :].astype(jnp.float32)

    sums = partial_ref[0:8, :], partial_ref[8:16, :]
    pixels = features_ref.shape[0]
    back = norm_back(own_ref, True, sums, read, table_ref, 0, pixels)
    count = own_ref.shape[0]
    own = pl.ds(pl.multiple_of(lax.axis_index("height") * count, count), count)
    total = residual_grad_ref[own, :] + back(own, slice(0, count))
    input_grad_ref[...] = total.astype(jnp.bfloat16)


def place_kernel(*refs):
    joints, packed_ref = refs[:-1], refs[-1]
    share = packed_ref.shape[0] // len(joints)
    me = lax.axis_index("canvas")
    for step, joint in enumerate(joints):
        place = pl.ds(pl.multiple_of((me ^ step) * share, share), share)
        packed_ref[place, :] = joint[...]


def spread_quarters(packed, flips, qkv_ref, proj_ref, qkv_hbm, proj_hbm, sems):
    quarter = packed[0].shape[0]
    inner = qkv_ref.shape[2]
    copies = []
    for index, packed_ref in enumerate(packed):
        owner = own_quarter() ^ flips[index]
        rows = pl.ds(pl.multiple_of(owner * quarter, quarter), quarter)
        qkv_ref[index] = packed_ref[:, 0:inner].astype(jnp.float32)
        proj_ref[index] = packed_ref[:, inner:].astype(jnp.float32)
        for which, (held, target) in enumerate(((qkv_ref, qkv_hbm), (proj_ref, proj_hbm))):
            copy = pltpu.make_async_copy(held.at[index], target.at[rows, :], sems.at[index, which])
            copy.start()
            copies.append(copy)
    return copies


def join_kernel(*refs):
    packed, (qkv_hbm, proj_hbm, qkv_ref, proj_ref, sems) = refs[:-5], refs[-5:]
    copies = spread_quarters(packed, [0, 2], qkv_ref, proj_ref, qkv_hbm, proj_hbm, sems)
    for copy in copies:
        copy.wait()


def halve_kernel(keep_ref, got_ref, hold_ref, send_ref):
    total = keep_ref[...].astype(jnp.float32) + got_ref[...].astype(jnp.float32)
    rows = hold_ref.shape[0]
    hold_ref[...] = total[0:rows]
    send_ref[0:rows, :] = total[rows:].astype(jnp.bfloat16)


def halve_sums_kernel(keep_ref, got_ref, sums_ref, got_sums_ref, hold_ref, send_ref, both_ref):
    halve_kernel(keep_ref, got_ref, hold_ref, send_ref)
    rows = hold_ref.shape[0]
    left = sums_ref[...] + got_sums_ref[...]
    both_ref[...] = left
    count, width = left.shape
    for part in range(2):
        low = left.astype(jnp.bfloat16)
        left = left - low.astype(jnp.float32)
        for block in range(width // LANES):
            send_ref[rows : rows + count, :] = low[:, block * LANES : (block + 1) * LANES]
            rows += count


def unpack_sums(got_ref, rows, count, width):
    total = jnp.zeros((count, width), jnp.float32)
    for part in range(2):
        blocks = []
        for block in range(width // LANES):
            blocks.append(got_ref[rows : rows + count, :].astype(jnp.float32))
            rows += count
        total = total + jnp.concatenate(blocks, axis=1)
    return total


def last_kernel(both_ref, old_qkv, old_proj, qkv_hbm, proj_hbm, qkv_ref, proj_ref, sems):
    copies = spread_quarters([both_ref], [3], qkv_ref, proj_ref, qkv_hbm, proj_hbm, sems)
    for copy in copies:
        copy.wait()


def sums_kernel(
    sums_ref,
    hold_ref,
    got_ref,
    chip_ref,
    old_qkv,
    old_proj,
    share_ref,
    gains_ref,
    shifts_ref,
    conv_ref,
    qv_ref,
    bias_ref,
    qkv_hbm,
    proj_hbm,
    qkv_ref,
    proj_ref,
    sems,
):
    copies = spread_quarters([chip_ref], [1], qkv_ref, proj_ref, qkv_hbm, proj_hbm, sems)
    rows = hold_ref.shape[0]
    total = hold_ref[...] + got_ref[0:rows, :].astype(jnp.float32)
    share_ref[...] = total.reshape(share_ref.shape)
    total = sums_ref[...]
    total = total + unpack_sums(got_ref, rows, *total.shape)
    for row, start in enumerate((0, 2, 5)):
        gains_ref[row : row + 1, :] = total[start : start + 1]
        shifts_ref[row : row + 1, :] = total[start + 1 : start + 2]
    conv_ref[0:1, :] = total[4:5]
    conv_ref[1:2, :] = total[7:8]
    qv_ref[...] = total[8:10]
    bias_ref[...] = total[10:11]
    for copy in copies:
        copy.wait()


def call_kernel(kernel, outputs, scratch, operands, places, flops, limit, out_places=None, aliases={}):
    out_places = out_places or "v" * len(outputs)
    spaces = {
        "v": pl.BlockSpec(memory_space=pltpu.VMEM),
        "s": pl.BlockSpec(memory_space=pltpu.SMEM),
        "h": pl.BlockSpec(memory_space=pl.ANY),
        "o": pl.BlockSpec(memory_space=pltpu.VMEM),
        "a": pl.BlockSpec(memory_space=pl.ANY),
    }
    moved = 8 * flops // LANES
    held = {"v": pltpu.VMEM, "h": pltpu.HBM, "o": jax.ShapeDtypeStruct}
    operands = [
        pltpu.with_memory_space_constraint(array, pltpu.HBM) if place == "h" else array
        for array, place in zip(operands, places)
    ]
    return pl.pallas_call(
        kernel,
        out_shape=[held[place](*output) for output, place in zip(outputs, out_places)],
        in_specs=[spaces[place] for place in places],
        out_specs=[spaces[place] for place in out_places],
        scratch_shapes=scratch,
        input_output_aliases=aliases,
        compiler_params=pltpu.CompilerParams(vmem_limit_bytes=limit * 2**20),
        cost_estimate=pl.CostEstimate(flops=flops, bytes_accessed=moved, transcendentals=0),
    )(*operands)


def send_height(block, step):
    size = lax.axis_size("height")
    return lax.ppermute(block, "height", [(i, i ^ step) for i in range(size)])


def with_cores(blocks):
    return [piece for block in blocks for piece in (block, send_height(block, 1))]


def send_canvas(block, step):
    size = lax.axis_size("canvas")
    return lax.ppermute(block, "canvas", [(i, i ^ step) for i in range(size)])


def send_phase(block, phase):
    canvases, size = lax.axis_size("canvas"), lax.axis_size("height")
    pairs = []
    for canvas in range(canvases):
        for height in range(size):
            step = 2 if (height ^ phase) & 1 else 1
            pairs.append((canvas * size + height, (canvas ^ step) * size + height))
    return lax.ppermute(block, ("canvas", "height"), pairs)


def trade_canvas(pieces):
    return [pieces[0]] + [send_canvas(piece, step) for step, piece in enumerate(pieces) if step]


def whole_canvas(
    features,
    tile_ids,
    norm_gains,
    norm_shifts,
    conv_weights,
    conv_biases,
    qkv_weight,
    qv_bias,
    proj_weight,
    proj_bias,
    cotangent,
):
    height_size = lax.axis_size("height")
    canvas_size = lax.axis_size("canvas")
    local_rows, cols, channels = features.shape[1:]
    all_rows = tile_ids.shape[1]
    pixels = all_rows * cols
    own_pixels = local_rows * cols
    out_share = channels // height_size
    ci_share = channels // canvas_size
    quarter = channels // 4
    row_share = quarter // canvas_size
    low, wide = jnp.bfloat16, jnp.float32

    own_features = features.reshape(own_pixels, channels)
    own_grad = cotangent.reshape(own_pixels, channels)
    steps = range(2, height_size, 2)
    held_features = [own_features] + [send_height(own_features, step) for step in steps]
    plane = ((pixels, channels), low)
    plane_wide = ((pixels, channels), wide)
    sums_shape = ((16, channels), wide)
    mixed_halves = [((2 * row_share, 4 * channels), low)] * 2
    taps = pltpu.VMEM((pixels + 2 * cols, 3 * channels), low)
    held_wide = pltpu.VMEM((pixels, channels), wide)
    flipped = pltpu.VMEM((channels, pixels), low)
    narrow = pltpu.VMEM((NARROW, pixels), low)
    columns = pltpu.VMEM((9 * out_share, pixels), low)
    part_held = pltpu.VMEM((9 * out_share, channels), low)
    sem = pltpu.SemaphoreType.DMA
    conv_flops = 2 * 9 * pixels * channels * channels
    dot_flops = 2 * pixels * channels * channels
    score_flops = 2 * pixels * pixels * channels
    scale = channels ** (-0.5)

    (
        held_conv,
        turned,
        held_qkv,
        held_proj,
        params,
        mask,
        lane_mask,
        id_rows,
        id_cols,
    ) = call_kernel(
        functools.partial(hold_kernel, cols=cols),
        [
            (conv_weights.shape, low),
            ((2, 3, channels, 3 * channels), low),
            (qkv_weight.shape, low),
            (proj_weight.shape, low),
            ((24, channels), wide),
            ((2, pixels, LANES), wide),
            ((8, pixels), wide),
            ((pixels, LANES), jnp.int32),
            ((8, pixels), jnp.int32),
        ],
        [
            pltpu.SMEM(tile_ids.shape, jnp.int32),
            pltpu.VMEM(norm_gains.shape, wide),
            pltpu.VMEM(norm_shifts.shape, wide),
            pltpu.VMEM(conv_biases.shape, wide),
            pltpu.VMEM(qv_bias.shape, wide),
            pltpu.VMEM((1, channels), wide),
            sem((27,)),
        ],
        [
            tile_ids,
            norm_gains,
            norm_shifts,
            conv_biases,
            conv_weights,
            qkv_weight,
            proj_weight,
            qv_bias,
            proj_bias.reshape(1, channels),
        ],
        "h" * 9,
        conv_flops,
        8,
    )
    held_features[1:] = [
        lax.optimization_barrier((params, block))[1] for block in held_features[1:]
    ]
    pieces = with_cores(held_features)
    far_grad, *pieces[4::2] = lax.optimization_barrier((own_grad, *held_features[2:]))
    held_grads = [own_grad, send_height(own_grad, 2)]
    held_grads[1], pieces[2] = lax.optimization_barrier((held_grads[1], held_features[1]))
    held_grads += [send_height(far_grad, step) for step in steps[1:]]

    all_features, act_one, middle, act_two, residual, table = call_kernel(
        functools.partial(conv_kernel, cols=cols, count=height_size),
        [plane, plane, plane_wide, plane, plane_wide, ((24, channels), wide)],
        [pltpu.VMEM((own_pixels, channels), low), taps, sem],
        [*pieces, held_conv, params, mask],
        "h" + "v" * (height_size + 2),
        2 * conv_flops,
        16,
    )
    residual, *held_grads = lax.optimization_barrier((residual, *held_grads))
    grad_pieces = with_cores(held_grads)
    normed, query, key, value, soft, out_flip, output = call_kernel(
        functools.partial(score_kernel, score_scale=scale),
        [
            plane,
            plane,
            plane,
            plane,
            ((pixels, pixels), low),
            ((channels, pixels), low),
            ((own_pixels, channels), low),
        ],
        [
            flipped,
            *[pltpu.VMEM((pixels, SCORE_ROWS), wide)] * (pixels // SCORE_ROWS),
        ],
        [
            held_qkv,
            held_proj,
            residual,
            table,
            id_rows,
            id_cols,
        ],
        "vvvvvv",
        3 * dot_flops + 2 * score_flops,
        20,
        "v" * 6 + "o",
    )
    normed, *grad_pieces = lax.optimization_barrier((normed, *grad_pieces))
    all_grad, packed, sums, keep_mixed, send_mixed = call_kernel(
        functools.partial(attention_kernel, score_scale=scale, count=height_size),
        [plane, ((pixels, 3 * channels), low), sums_shape, *mixed_halves],
        [
            pltpu.VMEM((quarter, 4 * channels), low),
            flipped,
            pltpu.VMEM((pixels, channels), low),
            pltpu.VMEM((pixels, pixels), low),
            pltpu.VMEM((quarter, pixels), low),
            sem((height_size,)),
            *[pltpu.VMEM((pixels, SCORE_ROWS), wide)] * (pixels // SCORE_ROWS),
        ],
        [held_proj, normed, query, key, value, soft, out_flip, *grad_pieces],
        "vvvvvvvh" + "a" * (height_size - 1),
        3 * dot_flops + 4 * score_flops,
        20,
    )
    got_mixed = send_phase(send_mixed, 0)
    residual_grad, grad_two, sums, part_two = call_kernel(
        functools.partial(third_kernel, cols=cols),
        [plane_wide, plane, sums_shape, ((9 * out_share, channels), low)],
        [held_wide, narrow, columns],
        [held_qkv, all_grad, packed, residual, table, act_two, lane_mask, sums],
        "vvvvvvvv",
        3 * dot_flops + conv_flops // height_size,
        16,
    )
    grad_two, got_mixed = lax.optimization_barrier((grad_two, got_mixed))
    hold_mixed, send_mixed = call_kernel(
        halve_kernel,
        [((row_share, 4 * channels), kind) for kind in (wide, low)],
        [],
        [keep_mixed, got_mixed],
        "vv",
        1,
        12,
    )
    got_mixed = send_phase(send_mixed, 1)
    grad_two, hold_mixed = lax.optimization_barrier((grad_two, hold_mixed))
    half_total, half_taps = call_kernel(
        functools.partial(turn_kernel, cols=cols),
        [plane_wide, (taps.shape, low)],
        [],
        [grad_two, mask, turned],
        "vvv",
        2 * conv_flops // 3,
        16,
    )
    half_total, got_mixed = lax.optimization_barrier((half_total, got_mixed))
    mixed_sum = (hold_mixed + got_mixed.astype(wide)).astype(low)
    joints = trade_canvas([mixed_sum] * canvas_size)
    halves = [((4 * 9 * out_share, ci_share), low)] * 2
    grad_one, sums, keep_share, send_share = call_kernel(
        functools.partial(second_kernel, cols=cols),
        [plane, sums_shape, *halves],
        [held_wide, narrow, columns, part_held, pltpu.VMEM((8, channels), wide)],
        [half_total, half_taps, middle, table, act_one, mask, lane_mask, turned, sums, part_two],
        "v" * 10,
        conv_flops // 2,
        20,
    )
    grad_one, *joints = lax.optimization_barrier((grad_one, *joints))
    (own_mixed,) = call_kernel(
        place_kernel,
        [((quarter, 4 * channels), low)],
        [],
        joints,
        "v" * canvas_size,
        1,
        12,
    )
    own_mixed, send_share = lax.optimization_barrier((own_mixed, send_share))
    chip_mixed = send_height(own_mixed, 2)
    core_mixed = send_height(own_mixed, 1)
    got_share = send_phase(send_share, 0)
    own_total, sums, partial_sums = call_kernel(
        functools.partial(first_kernel, cols=cols),
        [((own_pixels, channels), wide), sums_shape, sums_shape],
        [held_wide, taps],
        [grad_one, all_features, table, mask, sums, turned],
        "vvvvvv",
        1,
        20,
    )
    got_sums = send_phase(sums, 0)
    (input_grad,) = call_kernel(
        own_kernel,
        [((own_pixels, channels), low)],
        [],
        [own_total, partial_sums, all_features, residual_grad, table],
        "vvvvv",
        dot_flops // 4,
        12,
        "o",
    )
    input_grad, got_sums, core_mixed, got_share = lax.optimization_barrier(
        (input_grad, got_sums, core_mixed, got_share)
    )
    share_rows = 2 * 9 * out_share
    send_rows = share_rows + 2 * sums_shape[0][0] * channels // LANES
    hold_share, send_share, sums = call_kernel(
        halve_sums_kernel,
        [((share_rows, ci_share), wide), ((send_rows, ci_share), low), sums_shape],
        [],
        [keep_share, got_share, sums, got_sums],
        "vvvv",
        1,
        12,
    )
    got_share = send_phase(send_share, 1)

    def quarter_scratch(count):
        return [
            pltpu.VMEM((count, quarter, 3 * channels), wide),
            pltpu.VMEM((count, quarter, channels), wide),
            sem((count, 2)),
        ]

    grad_shapes = [(qkv_weight.shape, wide), (proj_weight.shape, wide)]
    core_mixed, hold_share = lax.optimization_barrier((core_mixed, hold_share))
    qkv_grad, proj_grad = call_kernel(
        join_kernel,
        grad_shapes,
        quarter_scratch(2),
        [own_mixed, core_mixed],
        "vv",
        conv_flops,
        12,
        "hh",
    )
    qkv_grad, chip_mixed, got_share = lax.optimization_barrier((qkv_grad, chip_mixed, got_share))
    both_mixed = send_height(chip_mixed, 1)
    vector_shapes = [norm_gains.shape, norm_shifts.shape, conv_biases.shape, qv_bias.shape]
    conv_grad, gains_grad, shifts_grad, biases_grad, qv_grad, proj_bias_grad, qkv_grad, proj_grad = (
        call_kernel(
            sums_kernel,
            [((2, 3, 3, out_share, ci_share), wide)]
            + [(shape, wide) for shape in vector_shapes + [(1, channels)]]
            + grad_shapes,
            quarter_scratch(1),
            [sums, hold_share, got_share, chip_mixed, qkv_grad, proj_grad],
            "vvvvhh",
            conv_flops,
            12,
            "oooooohh",
            {4: 6, 5: 7},
        )
    )
    conv_grad, both_mixed = lax.optimization_barrier((conv_grad, both_mixed))
    qkv_grad, proj_grad = call_kernel(
        last_kernel,
        grad_shapes,
        quarter_scratch(1),
        [both_mixed, qkv_grad, proj_grad],
        "vhh",
        1,
        12,
        "hh",
        {1: 0, 2: 1},
    )
    own_shape = (1, local_rows, cols, channels)
    return (
        output.reshape(own_shape),
        input_grad.reshape(own_shape),
        gains_grad,
        shifts_grad,
        jnp.swapaxes(conv_grad, 3, 4),
        biases_grad,
        qkv_grad,
        qv_grad,
        proj_grad,
        proj_bias_grad.reshape(channels),
    )


def on_device(*arrays):
    features, tile_ids = arrays[0], arrays[1]
    local_rows, cols, channels = features.shape[1:]
    pixels = tile_ids.shape[1] * cols
    height_size, canvas_size = lax.axis_size("height"), lax.axis_size("canvas")
    powers = all(size & (size - 1) == 0 for size in (height_size, canvas_size, cols))
    fits = (
        powers
        and height_size > 2
        and canvas_size == 4
        and channels == LANES * canvas_size
        and pixels <= MOST_PIXELS
        and pixels % FILL_ROWS == 0
        and FILL_ROWS % CHUNK == 0
        and pixels % SCORE_ROWS == 0
        and pixels % KEY_ROWS == 0
        and (local_rows * cols) % LANES == 0
        and CHUNK % cols == 0
        and cols % 16 == 0
        and channels % (LANES * canvas_size) == 0
        and 2 * channels == NARROW * height_size
    )
    return whole_canvas(*arrays) if fits else split_canvas(*arrays)


def solution(mesh):
    in_specs = (
        P("canvas", "height", None, None),
        P("canvas", None),
        P(),
        P(),
        P(),
        P(),
        P(),
        P(),
        P(),
        P(),
        P("canvas", "height", None, None),
    )
    out_specs = (
        P("canvas", "height", None, None),
        P("canvas", "height", None, None),
        P(),
        P(),
        P(None, None, None, "canvas", "height"),
        P(),
        P(),
        P(),
        P(),
        P(),
    )
    return jax.shard_map(
        on_device, mesh=mesh, in_specs=in_specs, out_specs=out_specs, check_vma=False
    )
```

```python
import functools

import jax
import jax.numpy as jnp
from jax import lax
from jax.experimental import pallas as pl
from jax.experimental.pallas import tpu as pltpu
from jax.sharding import PartitionSpec as P

GROUPS = 32


epsilon = 1e-06
masked_score = -1e30
MOST_PIXELS = 1024
LANES = 128
NARROW = 128
CHUNK = 128
FILL_ROWS = 256
QUERY_ROWS = 512
SCORE_ROWS = 256
KEY_ROWS = 256


def extended(block, sides, width):
    for axis, dim in sides:
        count = lax.axis_size(axis)
        forward = [(i, i + 1) for i in range(count - 1)]
        backward = [(target, source) for source, target in forward]
        low = lax.ppermute(
            lax.slice_in_dim(block, block.shape[dim] - width, None, axis=dim), axis, forward
        )
        high = lax.ppermute(lax.slice_in_dim(block, 0, width, axis=dim), axis, backward)
        block = jnp.concatenate([low, block, high], axis=dim)
    return block


def group_total(vector):
    return vector.reshape(GROUPS, -1).sum(axis=1)


def spread_groups(vector, channels):
    return jnp.repeat(vector, channels // GROUPS)


def norm_forward(values, gain, shift, members):
    channels = values.shape[1]
    totals = lax.psum(group_total(jnp.sum(values, axis=0)), "height")
    centered = values - spread_groups(totals / members, channels)
    squares = lax.psum(group_total(jnp.sum(centered * centered, axis=0)), "height")
    inverse = spread_groups(lax.rsqrt(squares / members + epsilon), channels)
    normed = centered * inverse
    return (normed, inverse, normed * gain + shift)


def norm_backward(grad_in, normed, inverse, gain, members):
    channels = grad_in.shape[1]
    scaled = grad_in * gain
    both_sums = lax.psum(
        (group_total(jnp.sum(scaled, axis=0)), group_total(jnp.sum(scaled * normed, axis=0))),
        "height",
    )
    mean_grad = spread_groups(both_sums[0] / members, channels)
    mean_cross = spread_groups(both_sums[1] / members, channels)
    result = inverse * (scaled - mean_grad - normed * mean_cross)
    return (result, jnp.sum(grad_in * normed, axis=0), jnp.sum(grad_in, axis=0))


def swish(values):
    return values * jax.nn.sigmoid(values)


def swish_slope(values):
    sigmoid_part = jax.nn.sigmoid(values)
    return sigmoid_part * (1.0 + values * (1.0 - sigmoid_part))


def tap_columns(padded, row_mask, local_rows, canvas_cols):
    pieces = []
    for row_tap in range(3):
        rows_taken = padded[row_tap : row_tap + local_rows] * row_mask[:, row_tap, None, None]
        for col_tap in range(3):
            pieces.append(rows_taken[:, col_tap : col_tap + canvas_cols])
    stacked = jnp.concatenate(pieces, axis=2)
    return stacked.reshape(local_rows * canvas_cols, stacked.shape[2])


def conv_forward(acts, row_mask, weight, bias):
    local_rows, canvas_cols, channels = acts.shape
    rimmed = extended(acts, (("height", 0),), 1)
    padded = jnp.pad(rimmed, ((0, 0), (1, 1), (0, 0)))
    gathered = tap_columns(padded, row_mask, local_rows, canvas_cols)
    result = (
        jnp.dot(
            gathered, weight.reshape(9 * channels, channels), preferred_element_type=jnp.float32
        )
        + bias
    )
    return (result, gathered)


def conv_backward(grad_low, row_mask, weight, gathered):
    local_rows, canvas_cols, channels = grad_low.shape
    flat_grad = grad_low.reshape(local_rows * canvas_cols, channels)
    weight_grad = lax.dot_general(
        gathered, flat_grad, (((0,), (0,)), ((), ())), preferred_element_type=jnp.float32
    )
    rimmed = extended(grad_low, (("height", 0),), 1)
    padded = jnp.pad(rimmed, ((0, 0), (1, 1), (0, 0)))
    grad_taps = tap_columns(padded, row_mask, local_rows, canvas_cols)
    flipped = jnp.transpose(weight[::-1, ::-1], (0, 1, 3, 2)).reshape(9 * channels, channels)
    input_part = jnp.dot(grad_taps, flipped, preferred_element_type=jnp.float32)
    return (
        input_part,
        weight_grad.reshape(3, 3, channels, channels),
        jnp.sum(flat_grad.astype(jnp.float32), axis=0),
    )


def take_rows(array, offset, count):
    return lax.dynamic_slice_in_dim(array, offset, count)


def score_grads(
    queries, out_grad, log_total, row_dots, query_ids, key_rows, value_rows, key_ids, score_scale
):
    scores = (
        lax.dot_general(
            queries, key_rows, (((1,), (1,)), ((), ())), preferred_element_type=jnp.float32
        )
        * score_scale
    )
    same_tile = query_ids[:, None] == key_ids[None, :]
    softmax_block = jnp.exp(jnp.where(same_tile, scores - log_total[:, None], masked_score))
    weight_grad = lax.dot_general(
        out_grad, value_rows, (((1,), (1,)), ((), ())), preferred_element_type=jnp.float32
    )
    score_grad = (softmax_block * (weight_grad - row_dots[:, None])).astype(jnp.bfloat16)
    return (softmax_block.astype(jnp.bfloat16), score_grad)


def split_canvas(
    features,
    tile_ids,
    norm_gains,
    norm_shifts,
    conv_weights,
    conv_biases,
    qkv_weight,
    qv_bias,
    proj_weight,
    proj_bias,
    cotangent,
):
    height_size = lax.axis_size("height")
    local_rows = features.shape[1]
    canvas_cols = features.shape[2]
    channels = features.shape[3]
    pixels = local_rows * canvas_cols
    row_ids = tile_ids[0]
    all_rows = row_ids.shape[0]
    members = float(all_rows * canvas_cols * (channels // GROUPS))
    score_scale = channels ** (-0.5)
    first_row = lax.axis_index("height") * local_rows
    edge_ids = jnp.full((1,), -1, jnp.int32)
    padded_ids = jnp.concatenate([edge_ids, row_ids, edge_ids])
    near_ids = lax.dynamic_slice_in_dim(padded_ids, first_row, local_rows + 2)
    own_rows = near_ids[1 : local_rows + 1]
    row_mask = jnp.stack(
        [near_ids[row_tap : row_tap + local_rows] == own_rows for row_tap in range(3)], axis=1
    ).astype(jnp.bfloat16)
    key_ids = jnp.repeat(row_ids, canvas_cols)
    query_ids = jnp.repeat(own_rows, canvas_cols)
    grid_shape = (local_rows, canvas_cols, channels)
    inputs = features[0].reshape(pixels, channels).astype(jnp.float32)
    normed_one, inverse_one, pre_one = norm_forward(inputs, norm_gains[0], norm_shifts[0], members)
    act_one = swish(pre_one).astype(jnp.bfloat16).reshape(grid_shape)
    middle, taps_one = conv_forward(act_one, row_mask, conv_weights[0], conv_biases[0])
    normed_two, inverse_two, pre_two = norm_forward(middle, norm_gains[1], norm_shifts[1], members)
    act_two = swish(pre_two).astype(jnp.bfloat16).reshape(grid_shape)
    branch, taps_two = conv_forward(act_two, row_mask, conv_weights[1], conv_biases[1])
    residual = inputs + branch
    normed_three, inverse_three, pre_three = norm_forward(
        residual, norm_gains[2], norm_shifts[2], members
    )
    attn_input = pre_three.astype(jnp.bfloat16)
    mixed = jnp.dot(attn_input, qkv_weight, preferred_element_type=jnp.float32)
    queries = (mixed[:, :channels] + qv_bias[0]).astype(jnp.bfloat16)
    key_rows = mixed[:, channels : 2 * channels].astype(jnp.bfloat16)
    value_rows = (mixed[:, 2 * channels :] + qv_bias[1]).astype(jnp.bfloat16)
    running_max = jnp.full((pixels,), masked_score, jnp.float32)
    key_piece = lax.all_gather(key_rows, "height", axis=0, tiled=True)
    value_piece = lax.all_gather(value_rows, "height", axis=0, tiled=True)
    scores = (
        lax.dot_general(
            queries, key_piece, (((1,), (1,)), ((), ())), preferred_element_type=jnp.float32
        )
        * score_scale
    )
    same_tile = query_ids[:, None] == key_ids[None, :]
    scores = jnp.where(same_tile, scores, masked_score)
    new_max = jnp.maximum(running_max, jnp.max(scores, axis=1))
    weights = jnp.where(same_tile, jnp.exp(scores - new_max[:, None]), 0.0)
    summed_out = jnp.dot(
        weights.astype(jnp.bfloat16), value_piece, preferred_element_type=jnp.float32
    )
    total_weight = jnp.sum(weights, axis=1)
    log_total = new_max + jnp.log(total_weight)
    attended = summed_out / total_weight[:, None]
    attended_low = attended.astype(jnp.bfloat16)
    output = (
        residual
        + jnp.dot(attended_low, proj_weight, preferred_element_type=jnp.float32)
        + proj_bias
    )
    out_grad = cotangent[0].reshape(pixels, channels)
    out_grad_full = out_grad.astype(jnp.float32)
    proj_grad = lax.dot_general(
        attended_low, out_grad, (((0,), (0,)), ((), ())), preferred_element_type=jnp.float32
    )
    proj_bias_grad = jnp.sum(out_grad_full, axis=0)
    attended_grad = lax.dot_general(
        out_grad, proj_weight, (((1,), (1,)), ((), ())), preferred_element_type=jnp.float32
    ).astype(jnp.bfloat16)
    row_dots = jnp.sum(attended_grad.astype(jnp.float32) * attended, axis=1)
    block_rows = pixels * min(height_size, 8)
    zero_block = jnp.zeros((pixels, channels), jnp.float32)
    key_all, value_all = (
        lax.all_gather(key_rows, "height", axis=0, tiled=True),
        lax.all_gather(value_rows, "height", axis=0, tiled=True),
    )
    query_all, grad_all = (
        lax.all_gather(queries, "height", axis=0, tiled=True),
        lax.all_gather(attended_grad, "height", axis=0, tiled=True),
    )
    total_all, dots_all = (
        lax.all_gather(log_total, "height", axis=0, tiled=True),
        lax.all_gather(row_dots, "height", axis=0, tiled=True),
    )

    def own_query_step(running, block_index):
        offset = block_index * block_rows
        key_part = take_rows(key_all, offset, block_rows)
        rounded, score_grad = score_grads(
            queries,
            attended_grad,
            log_total,
            row_dots,
            query_ids,
            key_part,
            take_rows(value_all, offset, block_rows),
            take_rows(key_ids, offset, block_rows),
            score_scale,
        )
        return (
            running
            + jnp.dot(score_grad, key_part, preferred_element_type=jnp.float32) * score_scale,
            None,
        )

    def own_key_step(running, block_index):
        offset = block_index * block_rows
        query_part = take_rows(query_all, offset, block_rows)
        grad_part = take_rows(grad_all, offset, block_rows)
        rounded, score_grad = score_grads(
            query_part,
            grad_part,
            take_rows(total_all, offset, block_rows),
            take_rows(dots_all, offset, block_rows),
            take_rows(key_ids, offset, block_rows),
            key_rows,
            value_rows,
            query_ids,
            score_scale,
        )
        key_part = (
            lax.dot_general(
                score_grad, query_part, (((0,), (0,)), ((), ())), preferred_element_type=jnp.float32
            )
            * score_scale
        )
        value_part = lax.dot_general(
            rounded, grad_part, (((0,), (0,)), ((), ())), preferred_element_type=jnp.float32
        )
        return ((running[0] + key_part, running[1] + value_part), None)

    block_count = key_all.shape[0] // block_rows
    query_grad, unused_one = lax.scan(own_query_step, zero_block, jnp.arange(block_count))
    (key_grad, value_grad), unused_two = lax.scan(
        own_key_step, (zero_block, zero_block), jnp.arange(block_count)
    )
    query_low = query_grad.astype(jnp.bfloat16)
    key_low = key_grad.astype(jnp.bfloat16)
    value_low = value_grad.astype(jnp.bfloat16)
    stacked_grad = jnp.concatenate([query_low, key_low, value_low], axis=1)
    qkv_grad = lax.dot_general(
        attn_input, stacked_grad, (((0,), (0,)), ((), ())), preferred_element_type=jnp.float32
    )
    qv_grad = jnp.stack(
        [
            jnp.sum(query_low.astype(jnp.float32), axis=0),
            jnp.sum(value_low.astype(jnp.float32), axis=0),
        ]
    )
    normed_grad = lax.dot_general(
        stacked_grad, qkv_weight, (((1,), (1,)), ((), ())), preferred_element_type=jnp.float32
    )
    back_three, gain_three, shift_three = norm_backward(
        normed_grad, normed_three, inverse_three, norm_gains[2], members
    )
    residual_grad = out_grad_full + back_three
    grad_two = residual_grad.astype(jnp.bfloat16).reshape(grid_shape)
    act_two_grad, weight_two_grad, bias_two_grad = conv_backward(
        grad_two, row_mask, conv_weights[1], taps_two
    )
    middle_grad, gain_two, shift_two = norm_backward(
        act_two_grad * swish_slope(pre_two), normed_two, inverse_two, norm_gains[1], members
    )
    grad_one = middle_grad.astype(jnp.bfloat16).reshape(grid_shape)
    act_one_grad, weight_one_grad, bias_one_grad = conv_backward(
        grad_one, row_mask, conv_weights[0], taps_one
    )
    input_back, gain_one, shift_one = norm_backward(
        act_one_grad * swish_slope(pre_one), normed_one, inverse_one, norm_gains[0], members
    )
    input_grad = residual_grad + input_back
    conv_grad = jnp.stack([weight_one_grad, weight_two_grad])
    conv_part = lax.psum_scatter(conv_grad, "height", scatter_dimension=4, tiled=True)
    conv_part = lax.psum_scatter(
        conv_part.astype(jnp.bfloat16), "canvas", scatter_dimension=3, tiled=True
    ).astype(jnp.float32)
    summed = lax.psum(
        (
            jnp.stack([gain_one, gain_two, gain_three]),
            jnp.stack([shift_one, shift_two, shift_three]),
            jnp.stack([bias_one_grad, bias_two_grad]),
            qkv_grad,
            qv_grad,
            proj_grad,
            proj_bias_grad,
        ),
        ("canvas", "height"),
    )
    return (
        output.astype(jnp.bfloat16).reshape((1,) + grid_shape),
        input_grad.astype(jnp.bfloat16).reshape((1,) + grid_shape),
        summed[0],
        summed[1],
        conv_part,
        summed[2],
        summed[3],
        summed[4],
        summed[5],
        summed[6],
    )


def fold(block):
    rows, width = block.shape
    return jnp.sum(block.reshape(rows // 8, 8, width), axis=0)


def group_lanes(block, group):
    lane = lax.broadcasted_iota(jnp.int32, block.shape, 1)
    width = block.shape[1]
    step = 1
    while step < group:
        above = pltpu.roll(block, step, 1)
        below = pltpu.roll(block, width - step, 1)
        block = block + jnp.where((lane & step) != 0, above, below)
        step *= 2
    return block


def group_mean(partial, members):
    spread = group_lanes(partial, partial.shape[1] // GROUPS)
    return jnp.sum(spread, axis=0, keepdims=True) * (1.0 / members)


def widen(block, width):
    return jnp.concatenate([block] * (width // block.shape[1]), axis=1)


def each_block(pixels, block, body, carry=0):
    def step(index, carry):
        return body(pl.ds(pl.multiple_of(index * block, block), block), carry)

    return lax.fori_loop(0, pixels // block, step, carry)


def each_chunk(pixels, body, carry):
    return each_block(pixels, CHUNK, body, carry)


def aligned(start, step):
    return start if isinstance(start, int) else pl.multiple_of(start, step)


class RunningStats:
    def __init__(self, channels):
        self.width = channels // GROUPS
        self.reference = None
        self.sums = self.squares = jnp.zeros((8, channels), jnp.float32)

    def add(self, block):
        if self.reference is None:
            self.reference = group_mean(block[0:8], 8.0 * self.width)
        offset = block - self.reference
        self.sums = self.sums + fold(offset)
        self.squares = self.squares + fold(offset * offset)

    def finish(self, pixels):
        both = group_lanes(jnp.concatenate([self.sums, self.squares], axis=0), self.width)
        share = 1.0 / (pixels * self.width)
        offset = column_total(both[0:8]) * share
        variance = column_total(both[8:16]) * share - offset * offset
        return self.reference + offset, lax.rsqrt(jnp.maximum(variance, 0.0) + epsilon)


def put_taps(taps_ref, block, rows, cols):
    count, channels = block.shape
    place = lax.broadcasted_iota(jnp.int32, block.shape, 0) & (cols - 1)
    left = jnp.where(place == 0, 0.0, pltpu.roll(block, 1, 0))
    right = jnp.where(place == cols - 1, 0.0, pltpu.roll(block, count - 1, 0))
    inner = pl.ds(aligned(rows.start + cols, cols), count)
    taps_ref[inner, 0:channels] = left.astype(jnp.bfloat16)
    taps_ref[inner, channels : 2 * channels] = block.astype(jnp.bfloat16)
    taps_ref[inner, 2 * channels :] = right.astype(jnp.bfloat16)


def clear_edges(taps_ref, cols):
    edge = jnp.zeros((cols, taps_ref.shape[1]), taps_ref.dtype)
    taps_ref[0:cols, :] = edge
    taps_ref[taps_ref.shape[0] - cols :, :] = edge


def begin_conv(taps_ref, product, total_ref, fill, first, cols):
    for start in range(0, total_ref.shape[0], FILL_ROWS):
        for inner in range(start, start + FILL_ROWS, CHUNK):
            fill(pl.ds(inner, CHUNK))
        rows = pl.ds(start, FILL_ROWS)
        total_ref[rows, :] = first(rows, product(taps_ref, pl.ds(start + cols, FILL_ROWS), 1))


def add_rows(taps_ref, product, mask_ref, total_ref, row_tap, last, cols, old_ref=None):
    pixels, channels = total_ref.shape
    old_ref = total_ref if old_ref is None else old_ref

    def step(rows, shifted):
        part = product(taps_ref, shifted, row_tap)
        mask = widen(mask_ref[row_tap // 2, rows, :], channels)
        value = old_ref[rows, :] + mask * part
        total_ref[rows, :] = value if last is None else last(rows, value)

    block = 2 * FILL_ROWS if last is None else FILL_ROWS
    for start in range(0, pixels, block):
        step(pl.ds(start, block), pl.ds(start + row_tap * cols, block))


def run_conv(taps_ref, product, mask_ref, total_ref, fill, first, last, cols):
    begin_conv(taps_ref, product, total_ref, fill, first, cols)
    add_rows(taps_ref, product, mask_ref, total_ref, 0, None, cols)
    add_rows(taps_ref, product, mask_ref, total_ref, 2, last, cols)


def product_forward(weight_ref):
    channels = weight_ref.shape[-1]

    def product(taps_ref, shifted, row_tap):
        return jnp.dot(
            taps_ref[shifted, :],
            weight_ref[row_tap].reshape(3 * channels, channels),
            preferred_element_type=jnp.float32,
        )

    return product


def product_backward(weight_ref):
    def product(taps_ref, shifted, row_tap):
        return lax.dot_general(
            taps_ref[shifted, :],
            weight_ref[row_tap],
            (((1,), (1,)), ((), ())),
            preferred_element_type=jnp.float32,
        )

    return product


def activation(read, mean, inverse, gain, shift, act_ref, taps_ref, cols):
    scale, offset = 0.5 * inverse * gain, 0.5 * shift

    def fill(rows):
        half = (read(rows) - mean) * scale + offset
        act = half * (1.0 + jnp.tanh(half))
        act_ref[rows, :] = act.astype(jnp.bfloat16)
        put_taps(taps_ref, act, rows, cols)

    return fill


def back_means(sums, gain, pixels):
    channels = gain.shape[1]
    members = float(pixels * (channels // GROUPS))
    return group_mean(sums[0] * gain, members), group_mean(sums[1] * gain, members)


def column_total(partial):
    return jnp.sum(partial, axis=0, keepdims=True)


def weight_part(act_ref, narrow, lanes_ref, flip_ref, columns_ref, part_ref, cols):
    pixels, channels = act_ref.shape
    height = lax.axis_index("height")
    share = NARROW // 2
    flip_ref[...] = narrow.T
    own = pl.ds(pl.multiple_of((height % 2) * share, share), share)
    grad = flip_ref[own, :].astype(jnp.float32)
    column = lax.broadcasted_iota(jnp.int32, grad.shape, 1) & (cols - 1)
    for col_tap in range(3):
        shifted = grad
        if col_tap == 0:
            shifted = jnp.where(column == cols - 1, 0.0, pltpu.roll(grad, pixels - 1, 1))
        elif col_tap == 2:
            shifted = jnp.where(column == 0, 0.0, pltpu.roll(grad, 1, 1))
        for row_tap in range(3):
            tap = 3 * row_tap + col_tap
            place = slice(tap * share, (tap + 1) * share)
            if row_tap == 1:
                columns_ref[place, :] = shifted.astype(jnp.bfloat16)
                continue
            side, turn = (0, pixels - cols) if row_tap == 0 else (1, cols)
            masked = (shifted * lanes_ref[side : side + 1, :]).astype(jnp.bfloat16)
            columns_ref[place, :] = pltpu.roll(masked, turn, 1)
    part_ref[...] = jnp.dot(
        columns_ref[...], act_ref[...], preferred_element_type=jnp.float32
    ).astype(jnp.bfloat16)


def begin_back(grad_ref, weights_ref, mask_ref, taps_ref, total_ref, cols):
    clear_edges(taps_ref, cols)

    def fill(rows):
        put_taps(taps_ref, grad_ref[rows, :].astype(jnp.float32), rows, cols)

    product = product_backward(weights_ref)
    begin_conv(taps_ref, product, total_ref, fill, lambda rows, part: part, cols)
    add_rows(taps_ref, product, mask_ref, total_ref, 0, None, cols)


def finish_back(
    weights_ref, mask_ref, taps_ref, total_ref, read, table_ref, which, cols, old_ref=None
):
    mean, inverse, gain, shift = norm_rows(table_ref, which)
    scale, offset = 0.5 * inverse * gain, 0.5 * shift
    sums = []

    def slope(rows, value):
        centered = read(rows) - mean
        half = centered * scale + offset
        turn = jnp.tanh(half)
        double = value * ((1.0 + turn) * (1.0 + half * (1.0 - turn)))
        sums.append((fold(double), fold(double * centered)))
        return double

    add_rows(
        taps_ref, product_backward(weights_ref), mask_ref, total_ref, 2, slope, cols, old_ref
    )
    plain, cross = sum(pair[0] for pair in sums), sum(pair[1] for pair in sums)
    return 0.5 * plain, 0.5 * inverse * cross


def norm_back(total_ref, double, sums, read, table_ref, which, pixels, scales_ref=None):
    mean, inverse, gain, shift = norm_rows(table_ref, which)
    mean_grad, mean_cross = back_means(sums, gain, pixels)
    slope = inverse * gain * (0.5 if double else 1.0)
    level, tilt = inverse * mean_grad, inverse * inverse * mean_cross
    if scales_ref is not None:
        for row, scales in enumerate((mean, slope, level, tilt)):
            scales_ref[row : row + 1, :] = scales

    def back(rows, inner):
        return total_ref[inner, :] * slope - level - (read(rows) - mean) * tilt

    return back


def own_lanes():
    block = lax.axis_index("height") // 2
    return pl.ds(pl.multiple_of(block * NARROW, NARROW), NARROW)


def narrow_back(total_ref, value_ref, scales_ref):
    lanes = own_lanes()
    mean, slope, level, tilt = (scales_ref[row : row + 1, lanes] for row in range(4))
    return total_ref[:, lanes] * slope - level - (value_ref[:, lanes] - mean) * tilt


def turn_kernel(grad_ref, mask_ref, weights_ref, total_ref, taps_ref, *, cols):
    begin_back(grad_ref, weights_ref.at[1], mask_ref, taps_ref, total_ref, cols)


def norm_rows(table_ref, which):
    picks = (2 * which, 2 * which + 1, 6 + which, 9 + which)
    return tuple(table_ref[pick : pick + 1, :] for pick in picks)


def build_masks(ids_ref, mask_ref, lanes_ref, id_rows_ref, id_cols_ref, cols):
    rows = ids_ref.shape[1]

    def one_row(row, carry):
        here = ids_ref[0, row]
        place = pl.ds(pl.multiple_of(row * cols, cols), cols)
        id_rows_ref[place, :] = jnp.full((cols, LANES), here, jnp.int32)
        for side, other in ((0, row - 1), (1, row + 1)):
            inside = jnp.logical_and(other >= 0, other < rows)
            other_id = ids_ref[0, jnp.clip(other, 0, rows - 1)]
            same = jnp.where(jnp.logical_and(inside, other_id == here), 1.0, 0.0)
            mask_ref[side, place, :] = jnp.full((cols, LANES), same, jnp.float32)
        return carry

    lax.fori_loop(0, rows, one_row, 0)
    lane = lax.broadcasted_iota(jnp.int32, (8, LANES), 1)
    each = LANES // cols
    for block in range(rows // each):
        ids = jnp.full((8, LANES), ids_ref[0, block * each], jnp.int32)
        for step in range(1, each):
            ids = jnp.where(lane >= step * cols, ids_ref[0, block * each + step], ids)
        id_cols_ref[:, block * LANES : (block + 1) * LANES] = ids
    ids = id_cols_ref[...].astype(jnp.float32)
    pixels = ids.shape[1]
    pixel = lax.broadcasted_iota(jnp.int32, ids.shape, 1)
    above = jnp.where(pixel < cols, -1.0, pltpu.roll(ids, cols, 1))
    below = jnp.where(pixel >= pixels - cols, -1.0, pltpu.roll(ids, pixels - cols, 1))
    lanes_ref[0:1, :] = jnp.where(above == ids, 1.0, 0.0)[0:1]
    lanes_ref[1:2, :] = jnp.where(below == ids, 1.0, 0.0)[0:1]


def place_pieces(pieces, whole_ref, sems):
    own_pixels = whole_ref.shape[0] // len(pieces)
    height = lax.axis_index("height")
    copies = []
    for place, piece in enumerate(pieces):
        start = pl.multiple_of((height ^ place) * own_pixels, own_pixels)
        rows = pl.ds(start, own_pixels)
        copies.append(pltpu.make_async_copy(piece, whole_ref.at[rows, :], sems.at[place]))
    return copies


def hold_kernel(
    ids_hbm,
    gains_hbm,
    shifts_hbm,
    biases_hbm,
    weights_hbm,
    qkv_hbm,
    proj_hbm,
    qv_bias_hbm,
    proj_bias_hbm,
    weights_ref,
    turned_ref,
    qkv_ref,
    proj_ref,
    table_ref,
    mask_ref,
    lanes_ref,
    id_rows_ref,
    id_cols_ref,
    ids_ref,
    gains_ref,
    shifts_ref,
    biases_ref,
    qv_bias_ref,
    proj_bias_ref,
    sems,
    *,
    cols,
):
    channels = weights_ref.shape[-1]
    small = [
        (ids_hbm, ids_ref),
        (gains_hbm, gains_ref),
        (shifts_hbm, shifts_ref),
        (biases_hbm, biases_ref),
        (qv_bias_hbm, qv_bias_ref),
        (proj_bias_hbm, proj_bias_ref),
    ]
    large = [(weights_hbm, weights_ref), (qkv_hbm, qkv_ref), (proj_hbm, proj_ref)]
    for which in range(2):
        for row_tap in range(3):
            for col_tap in range(3):
                place = slice(col_tap * channels, (col_tap + 1) * channels)
                large.append(
                    (
                        weights_hbm.at[which, 2 - row_tap, 2 - col_tap],
                        turned_ref.at[which, row_tap, :, place],
                    )
                )
    copies = [
        pltpu.make_async_copy(source, target, sems.at[index])
        for index, (source, target) in enumerate(small + large)
    ]
    for copy in copies:
        copy.start()
    for copy in copies[: len(small)]:
        copy.wait()
    build_masks(ids_ref, mask_ref, lanes_ref, id_rows_ref, id_cols_ref, cols)
    table_ref[6:9, :] = gains_ref[...]
    table_ref[9:12, :] = shifts_ref[...]
    table_ref[12:14, :] = biases_ref[...]
    table_ref[14:16, :] = qv_bias_ref[...]
    table_ref[16:17, :] = proj_bias_ref[...]
    for copy in copies[len(small) :]:
        copy.wait()


def conv_kernel(*refs, cols, count):
    pieces, refs = refs[:count], refs[count:]
    (
        weights_ref,
        params_ref,
        mask_ref,
        features_ref,
        act_one_ref,
        middle_ref,
        act_two_ref,
        residual_ref,
        table_ref,
        own_ref,
        taps_ref,
        sem,
    ) = refs
    pixels, channels = features_ref.shape
    wide = jnp.float32
    own_copy = pltpu.make_async_copy(pieces[0], own_ref, sem)
    own_copy.start()
    table_ref[...] = params_ref[...]
    clear_edges(taps_ref, cols)

    def read_input(rows):
        return features_ref[rows, :].astype(wide)

    def read_middle(rows):
        return middle_ref[rows, :]

    height = lax.axis_index("height")
    own_pixels = pixels // count
    seen = RunningStats(channels)
    for place in list(range(1, count)) + [0]:
        if place == 0:
            own_copy.wait()
        piece = (pieces[place] if place else own_ref)[...]
        start = pl.multiple_of((height ^ place) * own_pixels, own_pixels)
        features_ref[pl.ds(start, own_pixels), :] = piece
        seen.add(piece.astype(wide))
    table_ref[0:1, :], table_ref[1:2, :] = seen.finish(pixels)
    seen = RunningStats(channels)

    def keep(rows, value):
        seen.add(value)
        return value

    run_conv(
        taps_ref,
        product_forward(weights_ref.at[0]),
        mask_ref,
        middle_ref,
        activation(read_input, *norm_rows(table_ref, 0), act_one_ref, taps_ref, cols),
        lambda rows, part: part + table_ref[12:13, :],
        keep,
        cols,
    )
    table_ref[2:3, :], table_ref[3:4, :] = seen.finish(pixels)
    seen = RunningStats(channels)
    run_conv(
        taps_ref,
        product_forward(weights_ref.at[1]),
        mask_ref,
        residual_ref,
        activation(read_middle, *norm_rows(table_ref, 1), act_two_ref, taps_ref, cols),
        lambda rows, part: part + (read_input(rows) + table_ref[13:14, :]),
        keep,
        cols,
    )
    table_ref[4:5, :], table_ref[5:6, :] = seen.finish(pixels)


def score_kernel(
    qkv_ref,
    proj_ref,
    residual_ref,
    table_ref,
    id_rows_ref,
    id_cols_ref,
    normed_ref,
    query_ref,
    key_ref,
    value_ref,
    soft_ref,
    out_flip_ref,
    output_ref,
    value_flip_ref,
    *scores_refs,
    score_scale,
):
    pixels, channels = residual_ref.shape
    own_pixels = output_ref.shape[0]
    wide = jnp.float32
    exponent = score_scale * 1.4426950408889634
    mean, inverse, gain, shift = norm_rows(table_ref, 2)
    scale = inverse * gain

    def normalise(start):
        rows = slice(start, start + KEY_ROWS)
        normed = (residual_ref[rows, :] - mean) * scale + shift
        normed_ref[rows, :] = normed.astype(jnp.bfloat16)

    def project(start):
        rows = slice(start, start + KEY_ROWS)
        normed = normed_ref[rows, :]
        query_ref[rows, :] = (
            jnp.dot(normed, qkv_ref[:, 0:channels], preferred_element_type=wide)
            + table_ref[14:15, :]
        ).astype(jnp.bfloat16)
        key_ref[rows, :] = jnp.dot(
            normed, qkv_ref[:, channels : 2 * channels], preferred_element_type=wide
        ).astype(jnp.bfloat16)
        values = (
            jnp.dot(normed, qkv_ref[:, 2 * channels :], preferred_element_type=wide)
            + table_ref[15:16, :]
        ).astype(jnp.bfloat16)
        value_ref[rows, :] = values
        value_flip_ref[:, rows] = values.T

    normalise(0)
    for start in range(0, pixels, KEY_ROWS):
        if start + KEY_ROWS < pixels:
            normalise(start + KEY_ROWS)
        project(start)
    block = scores_refs[0].shape[1]
    steps = range(0, pixels, KEY_ROWS)

    def score(index):
        rows = slice(index * block, (index + 1) * block)
        for start in steps:
            keys = slice(start, start + KEY_ROWS)
            scores = lax.dot_general(
                key_ref[keys, :],
                query_ref[rows, :],
                (((1,), (1,)), ((), ())),
                preferred_element_type=wide,
            )
            same = widen(id_rows_ref[keys, :], block) == id_cols_ref[0:1, rows]
            scores_refs[index][keys, :] = jnp.where(same, scores, masked_score)

    def soften(index):
        rows = slice(index * block, (index + 1) * block)
        scores_ref = scores_refs[index]
        peak = jnp.full((8, block), masked_score, wide)
        for start in steps:
            scores = scores_ref[start : start + KEY_ROWS, :]
            peak = jnp.maximum(peak, jnp.max(scores.reshape(-1, 8, block), axis=0))
        peak = jnp.max(peak, axis=0, keepdims=True)
        total = jnp.zeros((8, block), wide)
        for start in steps:
            keys = slice(start, start + KEY_ROWS)
            powers = jnp.exp2((scores_ref[keys, :] - peak) * exponent)
            scores_ref[keys, :] = powers
            total = total + fold(powers)
        share = 1.0 / column_total(total)
        for start in steps:
            keys = slice(start, start + KEY_ROWS)
            soft_ref[keys, rows] = (scores_ref[keys, :] * share).astype(jnp.bfloat16)

    score(0)
    for index in range(len(scores_refs)):
        if index + 1 < len(scores_refs):
            score(index + 1)
        soften(index)

    def collect(rows, carry):
        out_flip_ref[rows, :] = jnp.dot(
            value_flip_ref[rows, :], soft_ref[...], preferred_element_type=wide
        ).astype(jnp.bfloat16)
        return carry

    each_block(channels, channels // 2, collect)
    height = lax.axis_index("height")
    own = pl.ds(pl.multiple_of(height * own_pixels, own_pixels), own_pixels)
    output_ref[...] = (
        residual_ref[own, :]
        + lax.dot_general(
            out_flip_ref[:, own],
            proj_ref[...],
            (((0,), (0,)), ((), ())),
            preferred_element_type=wide,
        )
        + table_ref[16:17, :]
    ).astype(jnp.bfloat16)


def own_quarter():
    height = lax.axis_index("height")
    return (height & 1) * 2 + ((height >> 1) & 1)


def attention_kernel(
    proj_ref,
    normed_ref,
    query_ref,
    key_ref,
    value_ref,
    soft_ref,
    out_flip_ref,
    *refs,
    score_scale,
    count,
):
    pieces, (grad_ref, packed_ref, sums_ref), refs = (
        refs[:count],
        refs[count : count + 3],
        refs[count + 3 :],
    )
    pixels, channels = normed_ref.shape
    blocks = pixels // SCORE_ROWS
    grads_refs, refs = refs[-blocks:], refs[:-blocks]
    keep_ref, send_ref, mixed_ref, key_flip_ref, back_ref, score_grad_ref, flip_ref, sems = refs
    wide = jnp.float32
    copies = place_pieces(pieces, grad_ref, sems)
    for copy in copies:
        copy.start()
    quarter = channels // 4
    own = pl.ds(pl.multiple_of(own_quarter() * quarter, quarter), quarter)
    flip_ref[...] = normed_ref[:, own].T
    key_flip_ref[...] = key_ref[...].T
    for copy in copies:
        copy.wait()
    block, count = SCORE_ROWS, blocks
    steps = range(0, pixels, KEY_ROWS)

    def block_rows(index):
        return slice(index * block, (index + 1) * block)

    for index in range(count):
        back_ref[block_rows(index), :] = lax.dot_general(
            grad_ref[block_rows(index), :],
            proj_ref[...],
            (((1,), (1,)), ((), ())),
            preferred_element_type=wide,
        ).astype(jnp.bfloat16)

    def weigh(index):
        total = jnp.zeros((8, block), wide)
        for start in steps:
            keys = slice(start, start + KEY_ROWS)
            weight_grad = lax.dot_general(
                value_ref[keys, :],
                back_ref[block_rows(index), :],
                (((1,), (1,)), ((), ())),
                preferred_element_type=wide,
            )
            grads_refs[index][keys, :] = weight_grad
            total = total + fold(soft_ref[keys, block_rows(index)].astype(wide) * weight_grad)
        return column_total(total)

    def slope(index, dots):
        for start in steps:
            keys = slice(start, start + KEY_ROWS)
            weights = soft_ref[keys, block_rows(index)].astype(wide)
            score_grad_ref[keys, block_rows(index)] = (
                weights * (grads_refs[index][keys, :] - dots)
            ).astype(jnp.bfloat16)

    dots = weigh(0)
    for index in range(count):
        now, rows = dots, block_rows(index)
        if index + 1 < count:
            dots = weigh(index + 1)
        slope(index, now)
        packed_ref[rows, 2 * channels :] = jnp.dot(
            soft_ref[rows, :], back_ref[...], preferred_element_type=wide
        ).astype(jnp.bfloat16)
        query_grad = jnp.dot(
            key_flip_ref[...], score_grad_ref[:, rows], preferred_element_type=wide
        )
        packed_ref[rows, 0:channels] = (query_grad * score_scale).astype(jnp.bfloat16).T
    for index in range(count):
        rows = block_rows(index)
        packed_ref[rows, channels : 2 * channels] = (
            jnp.dot(score_grad_ref[rows, :], query_ref[...], preferred_element_type=wide)
            * score_scale
        ).astype(jnp.bfloat16)

    def pack(rows, carry):
        return (
            carry[0] + fold(packed_ref[rows, 0:channels].astype(wide)),
            carry[1] + fold(packed_ref[rows, 2 * channels :].astype(wide)),
            carry[2] + fold(grad_ref[rows, :].astype(wide)),
        )

    zeros = jnp.zeros((8, channels), wide)
    totals = zeros, zeros, zeros
    for start in range(0, pixels, CHUNK):
        totals = pack(pl.ds(start, CHUNK), totals)
    sums_ref[...] = jnp.zeros(sums_ref.shape, wide)
    for row, total in enumerate(totals):
        sums_ref[8 + row : 9 + row, :] = column_total(total)
    mixed_ref[:, 0 : 3 * channels] = jnp.dot(
        flip_ref[...], packed_ref[...], preferred_element_type=wide
    ).astype(jnp.bfloat16)
    mixed_ref[:, 3 * channels :] = jnp.dot(
        out_flip_ref[own, :], grad_ref[...], preferred_element_type=wide
    ).astype(jnp.bfloat16)
    keep_half(mixed_ref, 0, keep_ref, send_ref)


def third_kernel(
    qkv_ref,
    grad_ref,
    packed_ref,
    residual_ref,
    table_ref,
    act_two_ref,
    lanes_ref,
    old_sums_ref,
    residual_grad_ref,
    grad_two_ref,
    sums_ref,
    part_ref,
    total_ref,
    flip_ref,
    columns_ref,
    *,
    cols,
):
    pixels, channels = residual_ref.shape
    block = FILL_ROWS
    wide = jnp.float32
    mean, inverse, gain, shift = norm_rows(table_ref, 2)
    zeros = jnp.zeros((8, channels), wide)

    sums = (zeros, zeros)
    for start in range(0, pixels, block):
        rows = pl.ds(start, block)
        normed_grad = lax.dot_general(
            packed_ref[rows, :], qkv_ref[...], (((1,), (1,)), ((), ())), preferred_element_type=wide
        )
        total_ref[rows, :] = normed_grad
        centered = residual_ref[rows, :] - mean
        sums = sums[0] + fold(normed_grad), sums[1] + fold(normed_grad * centered)
    sums = sums[0], sums[1] * inverse
    sums_ref[...] = old_sums_ref[...]
    sums_ref[5:6, :] = column_total(sums[1])
    sums_ref[6:7, :] = column_total(sums[0])
    back = norm_back(
        total_ref, False, sums, lambda rows: residual_ref[rows, :], table_ref, 2, pixels
    )

    def finish(rows, carry):
        total = grad_ref[rows, :].astype(wide) + back(rows, rows)
        residual_grad_ref[rows, :] = total
        low = total.astype(jnp.bfloat16)
        grad_two_ref[rows, :] = low
        return carry + fold(low.astype(wide))

    sums_ref[7:8, :] = column_total(each_chunk(pixels, finish, zeros))
    narrow = grad_two_ref[:, own_lanes()]
    weight_part(act_two_ref, narrow, lanes_ref, flip_ref, columns_ref, part_ref, cols)


def second_kernel(
    old_total_ref,
    taps_ref,
    middle_ref,
    table_ref,
    act_one_ref,
    mask_ref,
    lanes_ref,
    weights_ref,
    old_sums_ref,
    part_two_ref,
    grad_one_ref,
    sums_ref,
    keep_one_ref,
    send_one_ref,
    keep_two_ref,
    send_two_ref,
    total_ref,
    flip_ref,
    columns_ref,
    part_ref,
    scales_ref,
    *,
    cols,
):
    pixels, channels = middle_ref.shape

    def read(rows):
        return middle_ref[rows, :]

    sums = finish_back(
        weights_ref.at[1], mask_ref, taps_ref, total_ref, read, table_ref, 1, cols, old_total_ref
    )
    back = norm_back(total_ref, True, sums, read, table_ref, 1, pixels, scales_ref)
    narrow = narrow_back(total_ref, middle_ref, scales_ref).astype(jnp.bfloat16)
    weight_part(act_one_ref, narrow, lanes_ref, flip_ref, columns_ref, part_ref, cols)
    sums_ref[...] = old_sums_ref[...]
    sums_ref[2:3, :] = column_total(sums[1])
    sums_ref[3:4, :] = column_total(sums[0])

    def finish(rows, carry):
        low = back(rows, rows).astype(jnp.bfloat16)
        grad_one_ref[rows, :] = low
        return carry + fold(low.astype(jnp.float32))

    zeros = jnp.zeros((8, channels), jnp.float32)
    sums_ref[4:5, :] = column_total(each_chunk(pixels, finish, zeros))
    keep_half(part_ref, 1, keep_one_ref, send_one_ref)
    keep_half(part_two_ref, 1, keep_two_ref, send_two_ref)


def near_far():
    core = lax.axis_index("height") & 1
    return 1 + core, 2 - core


def keep_half(source_ref, axis, keep_ref, send_ref):
    me = lax.axis_index("canvas")
    near, far = near_far()
    rows, width = keep_ref.shape[0] // 2, keep_ref.shape[1]
    for target_ref, flip in ((keep_ref, 0), (send_ref, near)):
        for slot, other in enumerate((0, far)):
            owner = me ^ flip ^ other
            target = target_ref.at[slot * rows : (slot + 1) * rows, :]
            if axis == 0:
                target[...] = source_ref[pl.ds(pl.multiple_of(owner * rows, rows), rows), :]
            else:
                target[...] = source_ref[:, pl.ds(pl.multiple_of(owner * width, width), width)]


def first_kernel(
    grad_one_ref,
    features_ref,
    table_ref,
    mask_ref,
    old_sums_ref,
    weights_ref,
    own_ref,
    sums_ref,
    partial_ref,
    total_ref,
    taps_ref,
    *,
    cols,
):
    def read(rows):
        return features_ref[rows, :].astype(jnp.float32)

    weights = weights_ref.at[0]
    begin_back(grad_one_ref, weights, mask_ref, taps_ref, total_ref, cols)
    sums = finish_back(weights, mask_ref, taps_ref, total_ref, read, table_ref, 0, cols)
    partial_ref[0:8, :], partial_ref[8:16, :] = sums
    sums_ref[...] = old_sums_ref[...]
    sums_ref[0:1, :] = column_total(sums[1])
    sums_ref[1:2, :] = column_total(sums[0])
    count = own_ref.shape[0]
    own = pl.ds(pl.multiple_of(lax.axis_index("height") * count, count), count)
    own_ref[...] = total_ref[own, :]


def own_kernel(
    own_ref, partial_ref, features_ref, residual_grad_ref, table_ref, input_grad_ref
):
    def read(rows):
        return features_ref[rows, :].astype(jnp.float32)

    sums = partial_ref[0:8, :], partial_ref[8:16, :]
    pixels = features_ref.shape[0]
    back = norm_back(own_ref, True, sums, read, table_ref, 0, pixels)
    count = own_ref.shape[0]
    own = pl.ds(pl.multiple_of(lax.axis_index("height") * count, count), count)
    total = residual_grad_ref[own, :] + back(own, slice(0, count))
    input_grad_ref[...] = total.astype(jnp.bfloat16)


def place_kernel(*refs):
    joints, packed_ref = refs[:-1], refs[-1]
    share = packed_ref.shape[0] // len(joints)
    me = lax.axis_index("canvas")
    for step, joint in enumerate(joints):
        place = pl.ds(pl.multiple_of((me ^ step) * share, share), share)
        packed_ref[place, :] = joint[...]


def cut_kernel(packed_ref, *half_refs):
    rows = half_refs[0].shape[0]
    for index, half_ref in enumerate(half_refs):
        half_ref[...] = packed_ref[index * rows : (index + 1) * rows, :]


def spread_quarters(packed, flips, qkv_ref, proj_ref, qkv_hbm, proj_hbm, sems):
    quarter = packed[0].shape[0]
    inner = qkv_ref.shape[2]
    copies = []
    for index, packed_ref in enumerate(packed):
        owner = own_quarter() ^ flips[index]
        rows = pl.ds(pl.multiple_of(owner * quarter, quarter), quarter)
        qkv_ref[index] = packed_ref[:, 0:inner].astype(jnp.float32)
        proj_ref[index] = packed_ref[:, inner:].astype(jnp.float32)
        for which, (held, target) in enumerate(((qkv_ref, qkv_hbm), (proj_ref, proj_hbm))):
            copy = pltpu.make_async_copy(held.at[index], target.at[rows, :], sems.at[index, which])
            copy.start()
            copies.append(copy)
    return copies


def join_kernel(*refs):
    packed, (qkv_hbm, proj_hbm, qkv_ref, proj_ref, sems) = refs[:-5], refs[-5:]
    copies = spread_quarters(packed, [0, 2], qkv_ref, proj_ref, qkv_hbm, proj_hbm, sems)
    for copy in copies:
        copy.wait()


def halve_kernel(keep_ref, got_ref, hold_ref, send_ref):
    total = keep_ref[...].astype(jnp.float32) + got_ref[...].astype(jnp.float32)
    rows = hold_ref.shape[0]
    hold_ref[...] = total[0:rows]
    send_ref[0:rows, :] = total[rows:].astype(jnp.bfloat16)


def halve_sums_kernel(
    keep_ref,
    got_ref,
    keep_two_ref,
    got_two_ref,
    sums_ref,
    got_sums_ref,
    hold_ref,
    send_ref,
    hold_two_ref,
    both_ref,
):
    rows = hold_ref.shape[0]
    halve_kernel(keep_ref, got_ref, hold_ref, send_ref)
    halve_kernel(keep_two_ref, got_two_ref, hold_two_ref, send_ref.at[rows : 2 * rows, :])
    rows *= 2
    left = sums_ref[...] + got_sums_ref[...]
    both_ref[...] = left
    count, width = left.shape
    for part in range(2):
        low = left.astype(jnp.bfloat16)
        left = left - low.astype(jnp.float32)
        for block in range(width // LANES):
            send_ref[rows : rows + count, :] = low[:, block * LANES : (block + 1) * LANES]
            rows += count


def unpack_sums(got_ref, rows, count, width):
    total = jnp.zeros((count, width), jnp.float32)
    for part in range(2):
        blocks = []
        for block in range(width // LANES):
            blocks.append(got_ref[rows : rows + count, :].astype(jnp.float32))
            rows += count
        total = total + jnp.concatenate(blocks, axis=1)
    return total


def last_kernel(
    chip_ref,
    both_a_ref,
    both_b_ref,
    old_qkv,
    old_proj,
    qkv_hbm,
    proj_hbm,
    qkv_ref,
    proj_ref,
    sems,
):
    copies = []
    rows = both_a_ref.shape[0]
    inner = qkv_ref.shape[2]
    chips = (chip_ref.at[0:rows, :], chip_ref.at[rows : 2 * rows, :])
    for index, piece_ref in enumerate((*chips, both_a_ref, both_b_ref)):
        start = ((own_quarter() ^ (1 if index < 2 else 3)) * 2 + index % 2) * rows
        target = pl.ds(pl.multiple_of(start, rows), rows)
        qkv_ref[index] = piece_ref[:, 0:inner].astype(jnp.float32)
        proj_ref[index] = piece_ref[:, inner:].astype(jnp.float32)
        for which, (held, whole) in enumerate(((qkv_ref, qkv_hbm), (proj_ref, proj_hbm))):
            copy = pltpu.make_async_copy(held.at[index], whole.at[target, :], sems.at[index, which])
            copy.start()
            copies.append(copy)
    for copy in copies:
        copy.wait()


def sums_kernel(
    sums_ref,
    hold_one_ref,
    hold_two_ref,
    got_ref,
    share_ref,
    gains_ref,
    shifts_ref,
    conv_ref,
    qv_ref,
    bias_ref,
):
    rows = hold_one_ref.shape[0]
    for which, hold_ref in enumerate((hold_one_ref, hold_two_ref)):
        got = got_ref[which * rows : (which + 1) * rows, :].astype(jnp.float32)
        share_ref[which] = (hold_ref[...] + got).reshape(share_ref.shape[1:])
    total = sums_ref[...]
    total = total + unpack_sums(got_ref, 2 * rows, *total.shape)
    for row, start in enumerate((0, 2, 5)):
        gains_ref[row : row + 1, :] = total[start : start + 1]
        shifts_ref[row : row + 1, :] = total[start + 1 : start + 2]
    conv_ref[0:1, :] = total[4:5]
    conv_ref[1:2, :] = total[7:8]
    qv_ref[...] = total[8:10]
    bias_ref[...] = total[10:11]


def call_kernel(kernel, outputs, scratch, operands, places, flops, limit, out_places=None, aliases={}):
    out_places = out_places or "v" * len(outputs)
    spaces = {
        "v": pl.BlockSpec(memory_space=pltpu.VMEM),
        "s": pl.BlockSpec(memory_space=pltpu.SMEM),
        "h": pl.BlockSpec(memory_space=pl.ANY),
        "o": pl.BlockSpec(memory_space=pltpu.VMEM),
        "a": pl.BlockSpec(memory_space=pl.ANY),
    }
    moved = 8 * flops // LANES
    held = {"v": pltpu.VMEM, "h": pltpu.HBM, "o": jax.ShapeDtypeStruct}
    operands = [
        pltpu.with_memory_space_constraint(array, pltpu.HBM) if place == "h" else array
        for array, place in zip(operands, places)
    ]
    return pl.pallas_call(
        kernel,
        out_shape=[held[place](*output) for output, place in zip(outputs, out_places)],
        in_specs=[spaces[place] for place in places],
        out_specs=[spaces[place] for place in out_places],
        scratch_shapes=scratch,
        input_output_aliases=aliases,
        compiler_params=pltpu.CompilerParams(vmem_limit_bytes=limit * 2**20),
        cost_estimate=pl.CostEstimate(flops=flops, bytes_accessed=moved, transcendentals=0),
    )(*operands)


def send_height(block, step):
    size = lax.axis_size("height")
    return lax.ppermute(block, "height", [(i, i ^ step) for i in range(size)])


def with_cores(blocks):
    return [piece for block in blocks for piece in (block, send_height(block, 1))]


def send_canvas(block, step):
    size = lax.axis_size("canvas")
    return lax.ppermute(block, "canvas", [(i, i ^ step) for i in range(size)])


def send_phase(block, phase):
    canvases, size = lax.axis_size("canvas"), lax.axis_size("height")
    pairs = []
    for canvas in range(canvases):
        for height in range(size):
            step = 2 if (height ^ phase) & 1 else 1
            pairs.append((canvas * size + height, (canvas ^ step) * size + height))
    return lax.ppermute(block, ("canvas", "height"), pairs)


def trade_canvas(pieces):
    return [pieces[0]] + [send_canvas(piece, step) for step, piece in enumerate(pieces) if step]


def whole_canvas(
    features,
    tile_ids,
    norm_gains,
    norm_shifts,
    conv_weights,
    conv_biases,
    qkv_weight,
    qv_bias,
    proj_weight,
    proj_bias,
    cotangent,
):
    height_size = lax.axis_size("height")
    canvas_size = lax.axis_size("canvas")
    local_rows, cols, channels = features.shape[1:]
    all_rows = tile_ids.shape[1]
    pixels = all_rows * cols
    own_pixels = local_rows * cols
    out_share = channels // height_size
    ci_share = channels // canvas_size
    quarter = channels // 4
    row_share = quarter // canvas_size
    low, wide = jnp.bfloat16, jnp.float32

    own_features = features.reshape(own_pixels, channels)
    own_grad = cotangent.reshape(own_pixels, channels)
    steps = range(2, height_size, 2)
    held_features = [own_features] + [send_height(own_features, step) for step in steps]
    plane = ((pixels, channels), low)
    plane_wide = ((pixels, channels), wide)
    sums_shape = ((16, channels), wide)
    mixed_halves = [((2 * row_share, 4 * channels), low)] * 2
    taps = pltpu.VMEM((pixels + 2 * cols, 3 * channels), low)
    held_wide = pltpu.VMEM((pixels, channels), wide)
    flipped = pltpu.VMEM((channels, pixels), low)
    narrow = pltpu.VMEM((NARROW, pixels), low)
    columns = pltpu.VMEM((9 * out_share, pixels), low)
    part_held = pltpu.VMEM((9 * out_share, channels), low)
    sem = pltpu.SemaphoreType.DMA
    conv_flops = 2 * 9 * pixels * channels * channels
    dot_flops = 2 * pixels * channels * channels
    score_flops = 2 * pixels * pixels * channels
    scale = channels ** (-0.5)

    (
        held_conv,
        turned,
        held_qkv,
        held_proj,
        params,
        mask,
        lane_mask,
        id_rows,
        id_cols,
    ) = call_kernel(
        functools.partial(hold_kernel, cols=cols),
        [
            (conv_weights.shape, low),
            ((2, 3, channels, 3 * channels), low),
            (qkv_weight.shape, low),
            (proj_weight.shape, low),
            ((24, channels), wide),
            ((2, pixels, LANES), wide),
            ((8, pixels), wide),
            ((pixels, LANES), jnp.int32),
            ((8, pixels), jnp.int32),
        ],
        [
            pltpu.SMEM(tile_ids.shape, jnp.int32),
            pltpu.VMEM(norm_gains.shape, wide),
            pltpu.VMEM(norm_shifts.shape, wide),
            pltpu.VMEM(conv_biases.shape, wide),
            pltpu.VMEM(qv_bias.shape, wide),
            pltpu.VMEM((1, channels), wide),
            sem((27,)),
        ],
        [
            tile_ids,
            norm_gains,
            norm_shifts,
            conv_biases,
            conv_weights,
            qkv_weight,
            proj_weight,
            qv_bias,
            proj_bias.reshape(1, channels),
        ],
        "h" * 9,
        conv_flops,
        8,
    )
    held_features[1:] = [
        lax.optimization_barrier((params, block))[1] for block in held_features[1:]
    ]
    pieces = with_cores(held_features)
    far_grad, *pieces[4::2] = lax.optimization_barrier((own_grad, *held_features[2:]))
    held_grads = [own_grad, send_height(own_grad, 2)]
    held_grads[1], pieces[2] = lax.optimization_barrier((held_grads[1], held_features[1]))
    held_grads += [send_height(far_grad, step) for step in steps[1:]]

    all_features, act_one, middle, act_two, residual, table = call_kernel(
        functools.partial(conv_kernel, cols=cols, count=height_size),
        [plane, plane, plane_wide, plane, plane_wide, ((24, channels), wide)],
        [pltpu.VMEM((own_pixels, channels), low), taps, sem],
        [*pieces, held_conv, params, mask],
        "h" + "v" * (height_size + 2),
        2 * conv_flops,
        16,
    )
    residual, *held_grads = lax.optimization_barrier((residual, *held_grads))
    grad_pieces = with_cores(held_grads)
    normed, query, key, value, soft, out_flip, output = call_kernel(
        functools.partial(score_kernel, score_scale=scale),
        [
            plane,
            plane,
            plane,
            plane,
            ((pixels, pixels), low),
            ((channels, pixels), low),
            ((own_pixels, channels), low),
        ],
        [
            flipped,
            *[pltpu.VMEM((pixels, SCORE_ROWS), wide)] * (pixels // SCORE_ROWS),
        ],
        [
            held_qkv,
            held_proj,
            residual,
            table,
            id_rows,
            id_cols,
        ],
        "vvvvvv",
        3 * dot_flops + 2 * score_flops,
        20,
        "v" * 6 + "o",
    )
    normed, *grad_pieces = lax.optimization_barrier((normed, *grad_pieces))
    all_grad, packed, sums, keep_mixed, send_mixed = call_kernel(
        functools.partial(attention_kernel, score_scale=scale, count=height_size),
        [plane, ((pixels, 3 * channels), low), sums_shape, *mixed_halves],
        [
            pltpu.VMEM((quarter, 4 * channels), low),
            flipped,
            pltpu.VMEM((pixels, channels), low),
            pltpu.VMEM((pixels, pixels), low),
            pltpu.VMEM((quarter, pixels), low),
            sem((height_size,)),
            *[pltpu.VMEM((pixels, SCORE_ROWS), wide)] * (pixels // SCORE_ROWS),
        ],
        [held_proj, normed, query, key, value, soft, out_flip, *grad_pieces],
        "vvvvvvvh" + "a" * (height_size - 1),
        3 * dot_flops + 4 * score_flops,
        20,
    )
    got_mixed = send_phase(send_mixed, 0)
    residual_grad, grad_two, sums, part_two = call_kernel(
        functools.partial(third_kernel, cols=cols),
        [plane_wide, plane, sums_shape, ((9 * out_share, channels), low)],
        [held_wide, narrow, columns],
        [held_qkv, all_grad, packed, residual, table, act_two, lane_mask, sums],
        "vvvvvvvv",
        3 * dot_flops + conv_flops // height_size,
        16,
    )
    grad_two, got_mixed = lax.optimization_barrier((grad_two, got_mixed))
    hold_mixed, send_mixed = call_kernel(
        halve_kernel,
        [((row_share, 4 * channels), kind) for kind in (wide, low)],
        [],
        [keep_mixed, got_mixed],
        "vv",
        1,
        12,
    )
    got_mixed = send_phase(send_mixed, 1)
    grad_two, hold_mixed = lax.optimization_barrier((grad_two, hold_mixed))
    half_total, half_taps = call_kernel(
        functools.partial(turn_kernel, cols=cols),
        [plane_wide, (taps.shape, low)],
        [],
        [grad_two, mask, turned],
        "vvv",
        2 * conv_flops // 3,
        16,
    )
    half_total, got_mixed = lax.optimization_barrier((half_total, got_mixed))
    mixed_sum = (hold_mixed + got_mixed.astype(wide)).astype(low)
    joints = trade_canvas([mixed_sum] * canvas_size)
    halves = [((2 * 9 * out_share, ci_share), low)] * 4
    grad_one, sums, keep_one, send_one, keep_two, send_two = call_kernel(
        functools.partial(second_kernel, cols=cols),
        [plane, sums_shape, *halves],
        [held_wide, narrow, columns, part_held, pltpu.VMEM((8, channels), wide)],
        [half_total, half_taps, middle, table, act_one, mask, lane_mask, turned, sums, part_two],
        "v" * 10,
        conv_flops // 2,
        20,
    )
    grad_one, *joints = lax.optimization_barrier((grad_one, *joints))
    (own_mixed,) = call_kernel(
        place_kernel,
        [((quarter, 4 * channels), low)],
        [],
        joints,
        "v" * canvas_size,
        1,
        12,
    )
    own_mixed, send_one, send_two = lax.optimization_barrier((own_mixed, send_one, send_two))
    chip_mixed = send_height(own_mixed, 2)
    core_mixed = send_height(own_mixed, 1)
    got_one, got_two = send_phase(send_one, 0), send_phase(send_two, 0)
    own_total, sums, partial_sums = call_kernel(
        functools.partial(first_kernel, cols=cols),
        [((own_pixels, channels), wide), sums_shape, sums_shape],
        [held_wide, taps],
        [grad_one, all_features, table, mask, sums, turned],
        "vvvvvv",
        1,
        20,
    )
    got_sums = send_phase(sums, 0)
    (input_grad,) = call_kernel(
        own_kernel,
        [((own_pixels, channels), low)],
        [],
        [own_total, partial_sums, all_features, residual_grad, table],
        "vvvvv",
        dot_flops // 4,
        12,
        "o",
    )
    input_grad, got_sums, core_mixed, got_one, got_two = lax.optimization_barrier(
        (input_grad, got_sums, core_mixed, got_one, got_two)
    )
    share_rows = 9 * out_share
    send_rows = 2 * share_rows + 2 * sums_shape[0][0] * channels // LANES
    hold_one, send_share, hold_two, sums = call_kernel(
        halve_sums_kernel,
        [
            ((share_rows, ci_share), wide),
            ((send_rows, ci_share), low),
            ((share_rows, ci_share), wide),
            sums_shape,
        ],
        [],
        [keep_one, got_one, keep_two, got_two, sums, got_sums],
        "v" * 6,
        1,
        12,
    )
    got_share = send_phase(send_share, 1)

    def widened(count, rows):
        return [
            pltpu.VMEM((count, rows, 3 * channels), wide),
            pltpu.VMEM((count, rows, channels), wide),
            sem((count, 2)),
        ]

    grad_shapes = [(qkv_weight.shape, wide), (proj_weight.shape, wide)]
    core_mixed, hold_one = lax.optimization_barrier((core_mixed, hold_one))
    qkv_grad, proj_grad = call_kernel(
        join_kernel,
        grad_shapes,
        widened(2, quarter),
        [own_mixed, core_mixed],
        "vv",
        1,
        12,
        "hh",
    )
    qkv_grad, chip_mixed = lax.optimization_barrier((qkv_grad, chip_mixed))
    chip_halves = call_kernel(
        cut_kernel,
        [((quarter // 2, 4 * channels), low)] * 2,
        [],
        [chip_mixed],
        "v",
        1,
        12,
    )
    both_halves = [send_height(half, 1) for half in chip_halves]
    qkv_grad, proj_grad = call_kernel(
        last_kernel,
        grad_shapes,
        widened(4, quarter // 2),
        [chip_mixed, *both_halves, qkv_grad, proj_grad],
        "vvvhh",
        1,
        12,
        "hh",
        {3: 0, 4: 1},
    )
    qkv_grad, got_share = lax.optimization_barrier((qkv_grad, got_share))
    vector_shapes = [norm_gains.shape, norm_shifts.shape, conv_biases.shape, qv_bias.shape]
    conv_grad, gains_grad, shifts_grad, biases_grad, qv_grad, proj_bias_grad = call_kernel(
        sums_kernel,
        [((2, 3, 3, out_share, ci_share), wide)]
        + [(shape, wide) for shape in vector_shapes + [(1, channels)]],
        [],
        [sums, hold_one, hold_two, got_share],
        "vvvv",
        1,
        12,
        "o" * 6,
    )
    own_shape = (1, local_rows, cols, channels)
    return (
        output.reshape(own_shape),
        input_grad.reshape(own_shape),
        gains_grad,
        shifts_grad,
        jnp.swapaxes(conv_grad, 3, 4),
        biases_grad,
        qkv_grad,
        qv_grad,
        proj_grad,
        proj_bias_grad.reshape(channels),
    )


def on_device(*arrays):
    features, tile_ids = arrays[0], arrays[1]
    local_rows, cols, channels = features.shape[1:]
    pixels = tile_ids.shape[1] * cols
    height_size, canvas_size = lax.axis_size("height"), lax.axis_size("canvas")
    powers = all(size & (size - 1) == 0 for size in (height_size, canvas_size, cols))
    fits = (
        powers
        and height_size > 2
        and canvas_size == 4
        and channels == LANES * canvas_size
        and pixels <= MOST_PIXELS
        and pixels % FILL_ROWS == 0
        and FILL_ROWS % CHUNK == 0
        and pixels % SCORE_ROWS == 0
        and pixels % KEY_ROWS == 0
        and (local_rows * cols) % LANES == 0
        and CHUNK % cols == 0
        and cols % 16 == 0
        and channels % (LANES * canvas_size) == 0
        and 2 * channels == NARROW * height_size
    )
    return whole_canvas(*arrays) if fits else split_canvas(*arrays)


def solution(mesh):
    in_specs = (
        P("canvas", "height", None, None),
        P("canvas", None),
        P(),
        P(),
        P(),
        P(),
        P(),
        P(),
        P(),
        P(),
        P("canvas", "height", None, None),
    )
    out_specs = (
        P("canvas", "height", None, None),
        P("canvas", "height", None, None),
        P(),
        P(),
        P(None, None, None, "canvas", "height"),
        P(),
        P(),
        P(),
        P(),
        P(),
    )
    return jax.shard_map(
        on_device, mesh=mesh, in_specs=in_specs, out_specs=out_specs, check_vma=False
    )
```

```python
import functools

import jax
import jax.numpy as jnp
from jax import lax
from jax.experimental import pallas as pl
from jax.experimental.pallas import tpu as pltpu
from jax.sharding import PartitionSpec as P

GROUPS = 32


epsilon = 1e-06
masked_score = -1e30
MOST_PIXELS = 1024
LANES = 128
NARROW = 128
CHUNK = 128
FILL_ROWS = 256
QUERY_ROWS = 512
SCORE_ROWS = 256
KEY_ROWS = 256


def extended(block, sides, width):
    for axis, dim in sides:
        count = lax.axis_size(axis)
        forward = [(i, i + 1) for i in range(count - 1)]
        backward = [(target, source) for source, target in forward]
        low = lax.ppermute(
            lax.slice_in_dim(block, block.shape[dim] - width, None, axis=dim), axis, forward
        )
        high = lax.ppermute(lax.slice_in_dim(block, 0, width, axis=dim), axis, backward)
        block = jnp.concatenate([low, block, high], axis=dim)
    return block


def group_total(vector):
    return vector.reshape(GROUPS, -1).sum(axis=1)


def spread_groups(vector, channels):
    return jnp.repeat(vector, channels // GROUPS)


def norm_forward(values, gain, shift, members):
    channels = values.shape[1]
    totals = lax.psum(group_total(jnp.sum(values, axis=0)), "height")
    centered = values - spread_groups(totals / members, channels)
    squares = lax.psum(group_total(jnp.sum(centered * centered, axis=0)), "height")
    inverse = spread_groups(lax.rsqrt(squares / members + epsilon), channels)
    normed = centered * inverse
    return (normed, inverse, normed * gain + shift)


def norm_backward(grad_in, normed, inverse, gain, members):
    channels = grad_in.shape[1]
    scaled = grad_in * gain
    both_sums = lax.psum(
        (group_total(jnp.sum(scaled, axis=0)), group_total(jnp.sum(scaled * normed, axis=0))),
        "height",
    )
    mean_grad = spread_groups(both_sums[0] / members, channels)
    mean_cross = spread_groups(both_sums[1] / members, channels)
    result = inverse * (scaled - mean_grad - normed * mean_cross)
    return (result, jnp.sum(grad_in * normed, axis=0), jnp.sum(grad_in, axis=0))


def swish(values):
    return values * jax.nn.sigmoid(values)


def swish_slope(values):
    sigmoid_part = jax.nn.sigmoid(values)
    return sigmoid_part * (1.0 + values * (1.0 - sigmoid_part))


def tap_columns(padded, row_mask, local_rows, canvas_cols):
    pieces = []
    for row_tap in range(3):
        rows_taken = padded[row_tap : row_tap + local_rows] * row_mask[:, row_tap, None, None]
        for col_tap in range(3):
            pieces.append(rows_taken[:, col_tap : col_tap + canvas_cols])
    stacked = jnp.concatenate(pieces, axis=2)
    return stacked.reshape(local_rows * canvas_cols, stacked.shape[2])


def conv_forward(acts, row_mask, weight, bias):
    local_rows, canvas_cols, channels = acts.shape
    rimmed = extended(acts, (("height", 0),), 1)
    padded = jnp.pad(rimmed, ((0, 0), (1, 1), (0, 0)))
    gathered = tap_columns(padded, row_mask, local_rows, canvas_cols)
    result = (
        jnp.dot(
            gathered, weight.reshape(9 * channels, channels), preferred_element_type=jnp.float32
        )
        + bias
    )
    return (result, gathered)


def conv_backward(grad_low, row_mask, weight, gathered):
    local_rows, canvas_cols, channels = grad_low.shape
    flat_grad = grad_low.reshape(local_rows * canvas_cols, channels)
    weight_grad = lax.dot_general(
        gathered, flat_grad, (((0,), (0,)), ((), ())), preferred_element_type=jnp.float32
    )
    rimmed = extended(grad_low, (("height", 0),), 1)
    padded = jnp.pad(rimmed, ((0, 0), (1, 1), (0, 0)))
    grad_taps = tap_columns(padded, row_mask, local_rows, canvas_cols)
    flipped = jnp.transpose(weight[::-1, ::-1], (0, 1, 3, 2)).reshape(9 * channels, channels)
    input_part = jnp.dot(grad_taps, flipped, preferred_element_type=jnp.float32)
    return (
        input_part,
        weight_grad.reshape(3, 3, channels, channels),
        jnp.sum(flat_grad.astype(jnp.float32), axis=0),
    )


def take_rows(array, offset, count):
    return lax.dynamic_slice_in_dim(array, offset, count)


def score_grads(
    queries, out_grad, log_total, row_dots, query_ids, key_rows, value_rows, key_ids, score_scale
):
    scores = (
        lax.dot_general(
            queries, key_rows, (((1,), (1,)), ((), ())), preferred_element_type=jnp.float32
        )
        * score_scale
    )
    same_tile = query_ids[:, None] == key_ids[None, :]
    softmax_block = jnp.exp(jnp.where(same_tile, scores - log_total[:, None], masked_score))
    weight_grad = lax.dot_general(
        out_grad, value_rows, (((1,), (1,)), ((), ())), preferred_element_type=jnp.float32
    )
    score_grad = (softmax_block * (weight_grad - row_dots[:, None])).astype(jnp.bfloat16)
    return (softmax_block.astype(jnp.bfloat16), score_grad)


def split_canvas(
    features,
    tile_ids,
    norm_gains,
    norm_shifts,
    conv_weights,
    conv_biases,
    qkv_weight,
    qv_bias,
    proj_weight,
    proj_bias,
    cotangent,
):
    height_size = lax.axis_size("height")
    local_rows = features.shape[1]
    canvas_cols = features.shape[2]
    channels = features.shape[3]
    pixels = local_rows * canvas_cols
    row_ids = tile_ids[0]
    all_rows = row_ids.shape[0]
    members = float(all_rows * canvas_cols * (channels // GROUPS))
    score_scale = channels ** (-0.5)
    first_row = lax.axis_index("height") * local_rows
    edge_ids = jnp.full((1,), -1, jnp.int32)
    padded_ids = jnp.concatenate([edge_ids, row_ids, edge_ids])
    near_ids = lax.dynamic_slice_in_dim(padded_ids, first_row, local_rows + 2)
    own_rows = near_ids[1 : local_rows + 1]
    row_mask = jnp.stack(
        [near_ids[row_tap : row_tap + local_rows] == own_rows for row_tap in range(3)], axis=1
    ).astype(jnp.bfloat16)
    key_ids = jnp.repeat(row_ids, canvas_cols)
    query_ids = jnp.repeat(own_rows, canvas_cols)
    grid_shape = (local_rows, canvas_cols, channels)
    inputs = features[0].reshape(pixels, channels).astype(jnp.float32)
    normed_one, inverse_one, pre_one = norm_forward(inputs, norm_gains[0], norm_shifts[0], members)
    act_one = swish(pre_one).astype(jnp.bfloat16).reshape(grid_shape)
    middle, taps_one = conv_forward(act_one, row_mask, conv_weights[0], conv_biases[0])
    normed_two, inverse_two, pre_two = norm_forward(middle, norm_gains[1], norm_shifts[1], members)
    act_two = swish(pre_two).astype(jnp.bfloat16).reshape(grid_shape)
    branch, taps_two = conv_forward(act_two, row_mask, conv_weights[1], conv_biases[1])
    residual = inputs + branch
    normed_three, inverse_three, pre_three = norm_forward(
        residual, norm_gains[2], norm_shifts[2], members
    )
    attn_input = pre_three.astype(jnp.bfloat16)
    mixed = jnp.dot(attn_input, qkv_weight, preferred_element_type=jnp.float32)
    queries = (mixed[:, :channels] + qv_bias[0]).astype(jnp.bfloat16)
    key_rows = mixed[:, channels : 2 * channels].astype(jnp.bfloat16)
    value_rows = (mixed[:, 2 * channels :] + qv_bias[1]).astype(jnp.bfloat16)
    running_max = jnp.full((pixels,), masked_score, jnp.float32)
    key_piece = lax.all_gather(key_rows, "height", axis=0, tiled=True)
    value_piece = lax.all_gather(value_rows, "height", axis=0, tiled=True)
    scores = (
        lax.dot_general(
            queries, key_piece, (((1,), (1,)), ((), ())), preferred_element_type=jnp.float32
        )
        * score_scale
    )
    same_tile = query_ids[:, None] == key_ids[None, :]
    scores = jnp.where(same_tile, scores, masked_score)
    new_max = jnp.maximum(running_max, jnp.max(scores, axis=1))
    weights = jnp.where(same_tile, jnp.exp(scores - new_max[:, None]), 0.0)
    summed_out = jnp.dot(
        weights.astype(jnp.bfloat16), value_piece, preferred_element_type=jnp.float32
    )
    total_weight = jnp.sum(weights, axis=1)
    log_total = new_max + jnp.log(total_weight)
    attended = summed_out / total_weight[:, None]
    attended_low = attended.astype(jnp.bfloat16)
    output = (
        residual
        + jnp.dot(attended_low, proj_weight, preferred_element_type=jnp.float32)
        + proj_bias
    )
    out_grad = cotangent[0].reshape(pixels, channels)
    out_grad_full = out_grad.astype(jnp.float32)
    proj_grad = lax.dot_general(
        attended_low, out_grad, (((0,), (0,)), ((), ())), preferred_element_type=jnp.float32
    )
    proj_bias_grad = jnp.sum(out_grad_full, axis=0)
    attended_grad = lax.dot_general(
        out_grad, proj_weight, (((1,), (1,)), ((), ())), preferred_element_type=jnp.float32
    ).astype(jnp.bfloat16)
    row_dots = jnp.sum(attended_grad.astype(jnp.float32) * attended, axis=1)
    block_rows = pixels * min(height_size, 8)
    zero_block = jnp.zeros((pixels, channels), jnp.float32)
    key_all, value_all = (
        lax.all_gather(key_rows, "height", axis=0, tiled=True),
        lax.all_gather(value_rows, "height", axis=0, tiled=True),
    )
    query_all, grad_all = (
        lax.all_gather(queries, "height", axis=0, tiled=True),
        lax.all_gather(attended_grad, "height", axis=0, tiled=True),
    )
    total_all, dots_all = (
        lax.all_gather(log_total, "height", axis=0, tiled=True),
        lax.all_gather(row_dots, "height", axis=0, tiled=True),
    )

    def own_query_step(running, block_index):
        offset = block_index * block_rows
        key_part = take_rows(key_all, offset, block_rows)
        rounded, score_grad = score_grads(
            queries,
            attended_grad,
            log_total,
            row_dots,
            query_ids,
            key_part,
            take_rows(value_all, offset, block_rows),
            take_rows(key_ids, offset, block_rows),
            score_scale,
        )
        return (
            running
            + jnp.dot(score_grad, key_part, preferred_element_type=jnp.float32) * score_scale,
            None,
        )

    def own_key_step(running, block_index):
        offset = block_index * block_rows
        query_part = take_rows(query_all, offset, block_rows)
        grad_part = take_rows(grad_all, offset, block_rows)
        rounded, score_grad = score_grads(
            query_part,
            grad_part,
            take_rows(total_all, offset, block_rows),
            take_rows(dots_all, offset, block_rows),
            take_rows(key_ids, offset, block_rows),
            key_rows,
            value_rows,
            query_ids,
            score_scale,
        )
        key_part = (
            lax.dot_general(
                score_grad, query_part, (((0,), (0,)), ((), ())), preferred_element_type=jnp.float32
            )
            * score_scale
        )
        value_part = lax.dot_general(
            rounded, grad_part, (((0,), (0,)), ((), ())), preferred_element_type=jnp.float32
        )
        return ((running[0] + key_part, running[1] + value_part), None)

    block_count = key_all.shape[0] // block_rows
    query_grad, unused_one = lax.scan(own_query_step, zero_block, jnp.arange(block_count))
    (key_grad, value_grad), unused_two = lax.scan(
        own_key_step, (zero_block, zero_block), jnp.arange(block_count)
    )
    query_low = query_grad.astype(jnp.bfloat16)
    key_low = key_grad.astype(jnp.bfloat16)
    value_low = value_grad.astype(jnp.bfloat16)
    stacked_grad = jnp.concatenate([query_low, key_low, value_low], axis=1)
    qkv_grad = lax.dot_general(
        attn_input, stacked_grad, (((0,), (0,)), ((), ())), preferred_element_type=jnp.float32
    )
    qv_grad = jnp.stack(
        [
            jnp.sum(query_low.astype(jnp.float32), axis=0),
            jnp.sum(value_low.astype(jnp.float32), axis=0),
        ]
    )
    normed_grad = lax.dot_general(
        stacked_grad, qkv_weight, (((1,), (1,)), ((), ())), preferred_element_type=jnp.float32
    )
    back_three, gain_three, shift_three = norm_backward(
        normed_grad, normed_three, inverse_three, norm_gains[2], members
    )
    residual_grad = out_grad_full + back_three
    grad_two = residual_grad.astype(jnp.bfloat16).reshape(grid_shape)
    act_two_grad, weight_two_grad, bias_two_grad = conv_backward(
        grad_two, row_mask, conv_weights[1], taps_two
    )
    middle_grad, gain_two, shift_two = norm_backward(
        act_two_grad * swish_slope(pre_two), normed_two, inverse_two, norm_gains[1], members
    )
    grad_one = middle_grad.astype(jnp.bfloat16).reshape(grid_shape)
    act_one_grad, weight_one_grad, bias_one_grad = conv_backward(
        grad_one, row_mask, conv_weights[0], taps_one
    )
    input_back, gain_one, shift_one = norm_backward(
        act_one_grad * swish_slope(pre_one), normed_one, inverse_one, norm_gains[0], members
    )
    input_grad = residual_grad + input_back
    conv_grad = jnp.stack([weight_one_grad, weight_two_grad])
    conv_part = lax.psum_scatter(conv_grad, "height", scatter_dimension=4, tiled=True)
    conv_part = lax.psum_scatter(
        conv_part.astype(jnp.bfloat16), "canvas", scatter_dimension=3, tiled=True
    ).astype(jnp.float32)
    summed = lax.psum(
        (
            jnp.stack([gain_one, gain_two, gain_three]),
            jnp.stack([shift_one, shift_two, shift_three]),
            jnp.stack([bias_one_grad, bias_two_grad]),
            qkv_grad,
            qv_grad,
            proj_grad,
            proj_bias_grad,
        ),
        ("canvas", "height"),
    )
    return (
        output.astype(jnp.bfloat16).reshape((1,) + grid_shape),
        input_grad.astype(jnp.bfloat16).reshape((1,) + grid_shape),
        summed[0],
        summed[1],
        conv_part,
        summed[2],
        summed[3],
        summed[4],
        summed[5],
        summed[6],
    )


def fold(block):
    rows, width = block.shape
    return jnp.sum(block.reshape(rows // 8, 8, width), axis=0)


def group_lanes(block, group):
    lane = lax.broadcasted_iota(jnp.int32, block.shape, 1)
    width = block.shape[1]
    step = 1
    while step < group:
        above = pltpu.roll(block, step, 1)
        below = pltpu.roll(block, width - step, 1)
        block = block + jnp.where((lane & step) != 0, above, below)
        step *= 2
    return block


def group_mean(partial, members):
    spread = group_lanes(partial, partial.shape[1] // GROUPS)
    return jnp.sum(spread, axis=0, keepdims=True) * (1.0 / members)


def widen(block, width):
    return jnp.concatenate([block] * (width // block.shape[1]), axis=1)


def each_block(pixels, block, body, carry=0):
    def step(index, carry):
        return body(pl.ds(pl.multiple_of(index * block, block), block), carry)

    return lax.fori_loop(0, pixels // block, step, carry)


def each_chunk(pixels, body, carry):
    return each_block(pixels, CHUNK, body, carry)


def aligned(start, step):
    return start if isinstance(start, int) else pl.multiple_of(start, step)


class RunningStats:
    def __init__(self, channels):
        self.width = channels // GROUPS
        self.reference = None
        self.sums = self.squares = jnp.zeros((8, channels), jnp.float32)

    def add(self, block):
        if self.reference is None:
            self.reference = group_mean(block[0:8], 8.0 * self.width)
        offset = block - self.reference
        self.sums = self.sums + fold(offset)
        self.squares = self.squares + fold(offset * offset)

    def finish(self, pixels):
        both = group_lanes(jnp.concatenate([self.sums, self.squares], axis=0), self.width)
        share = 1.0 / (pixels * self.width)
        offset = column_total(both[0:8]) * share
        variance = column_total(both[8:16]) * share - offset * offset
        return self.reference + offset, lax.rsqrt(jnp.maximum(variance, 0.0) + epsilon)


def put_taps(taps_ref, block, rows, cols):
    count, channels = block.shape
    place = lax.broadcasted_iota(jnp.int32, block.shape, 0) & (cols - 1)
    left = jnp.where(place == 0, 0.0, pltpu.roll(block, 1, 0))
    right = jnp.where(place == cols - 1, 0.0, pltpu.roll(block, count - 1, 0))
    inner = pl.ds(aligned(rows.start + cols, cols), count)
    taps_ref[inner, 0:channels] = left.astype(jnp.bfloat16)
    taps_ref[inner, channels : 2 * channels] = block.astype(jnp.bfloat16)
    taps_ref[inner, 2 * channels :] = right.astype(jnp.bfloat16)


def clear_edges(taps_ref, cols):
    edge = jnp.zeros((cols, taps_ref.shape[1]), taps_ref.dtype)
    taps_ref[0:cols, :] = edge
    taps_ref[taps_ref.shape[0] - cols :, :] = edge


def begin_conv(taps_ref, product, total_ref, fill, first, cols):
    for start in range(0, total_ref.shape[0], FILL_ROWS):
        for inner in range(start, start + FILL_ROWS, CHUNK):
            fill(pl.ds(inner, CHUNK))
        rows = pl.ds(start, FILL_ROWS)
        total_ref[rows, :] = first(rows, product(taps_ref, pl.ds(start + cols, FILL_ROWS), 1))


def add_rows(taps_ref, product, mask_ref, total_ref, row_tap, last, cols, old_ref=None):
    pixels, channels = total_ref.shape
    old_ref = total_ref if old_ref is None else old_ref

    def step(rows, shifted):
        part = product(taps_ref, shifted, row_tap)
        mask = widen(mask_ref[row_tap // 2, rows, :], channels)
        value = old_ref[rows, :] + mask * part
        total_ref[rows, :] = value if last is None else last(rows, value)

    block = 2 * FILL_ROWS if last is None else FILL_ROWS
    for start in range(0, pixels, block):
        step(pl.ds(start, block), pl.ds(start + row_tap * cols, block))


def run_conv(taps_ref, product, mask_ref, total_ref, fill, first, last, cols):
    begin_conv(taps_ref, product, total_ref, fill, first, cols)
    add_rows(taps_ref, product, mask_ref, total_ref, 0, None, cols)
    add_rows(taps_ref, product, mask_ref, total_ref, 2, last, cols)


def product_forward(weight_ref):
    channels = weight_ref.shape[-1]

    def product(taps_ref, shifted, row_tap):
        return jnp.dot(
            taps_ref[shifted, :],
            weight_ref[row_tap].reshape(3 * channels, channels),
            preferred_element_type=jnp.float32,
        )

    return product


def product_backward(weight_ref):
    def product(taps_ref, shifted, row_tap):
        return lax.dot_general(
            taps_ref[shifted, :],
            weight_ref[row_tap],
            (((1,), (1,)), ((), ())),
            preferred_element_type=jnp.float32,
        )

    return product


def activation(read, mean, inverse, gain, shift, act_ref, taps_ref, cols):
    scale, offset = 0.5 * inverse * gain, 0.5 * shift

    def fill(rows):
        half = (read(rows) - mean) * scale + offset
        act = half * (1.0 + jnp.tanh(half))
        act_ref[rows, :] = act.astype(jnp.bfloat16)
        put_taps(taps_ref, act, rows, cols)

    return fill


def back_means(sums, gain, pixels):
    channels = gain.shape[1]
    members = float(pixels * (channels // GROUPS))
    return group_mean(sums[0] * gain, members), group_mean(sums[1] * gain, members)


def column_total(partial):
    return jnp.sum(partial, axis=0, keepdims=True)


def weight_part(act_ref, narrow, lanes_ref, flip_ref, columns_ref, part_ref, cols):
    pixels, channels = act_ref.shape
    height = lax.axis_index("height")
    share = NARROW // 2
    flip_ref[...] = narrow.T
    own = pl.ds(pl.multiple_of((height % 2) * share, share), share)
    grad = flip_ref[own, :].astype(jnp.float32)
    column = lax.broadcasted_iota(jnp.int32, grad.shape, 1) & (cols - 1)
    for col_tap in range(3):
        shifted = grad
        if col_tap == 0:
            shifted = jnp.where(column == cols - 1, 0.0, pltpu.roll(grad, pixels - 1, 1))
        elif col_tap == 2:
            shifted = jnp.where(column == 0, 0.0, pltpu.roll(grad, 1, 1))
        for row_tap in range(3):
            tap = 3 * row_tap + col_tap
            place = slice(tap * share, (tap + 1) * share)
            if row_tap == 1:
                columns_ref[place, :] = shifted.astype(jnp.bfloat16)
                continue
            side, turn = (0, pixels - cols) if row_tap == 0 else (1, cols)
            masked = (shifted * lanes_ref[side : side + 1, :]).astype(jnp.bfloat16)
            columns_ref[place, :] = pltpu.roll(masked, turn, 1)
    part_ref[...] = jnp.dot(
        columns_ref[...], act_ref[...], preferred_element_type=jnp.float32
    ).astype(jnp.bfloat16)


def begin_back(grad_ref, weights_ref, mask_ref, taps_ref, total_ref, cols):
    clear_edges(taps_ref, cols)

    def fill(rows):
        put_taps(taps_ref, grad_ref[rows, :].astype(jnp.float32), rows, cols)

    product = product_backward(weights_ref)
    begin_conv(taps_ref, product, total_ref, fill, lambda rows, part: part, cols)
    add_rows(taps_ref, product, mask_ref, total_ref, 0, None, cols)


def finish_back(
    weights_ref, mask_ref, taps_ref, total_ref, read, table_ref, which, cols, old_ref=None
):
    mean, inverse, gain, shift = norm_rows(table_ref, which)
    scale, offset = 0.5 * inverse * gain, 0.5 * shift
    sums = []

    def slope(rows, value):
        centered = read(rows) - mean
        half = centered * scale + offset
        turn = jnp.tanh(half)
        double = value * ((1.0 + turn) * (1.0 + half * (1.0 - turn)))
        sums.append((fold(double), fold(double * centered)))
        return double

    add_rows(
        taps_ref, product_backward(weights_ref), mask_ref, total_ref, 2, slope, cols, old_ref
    )
    plain, cross = sum(pair[0] for pair in sums), sum(pair[1] for pair in sums)
    return 0.5 * plain, 0.5 * inverse * cross


def norm_back(total_ref, double, sums, read, table_ref, which, pixels, scales_ref=None):
    mean, inverse, gain, shift = norm_rows(table_ref, which)
    mean_grad, mean_cross = back_means(sums, gain, pixels)
    slope = inverse * gain * (0.5 if double else 1.0)
    level, tilt = inverse * mean_grad, inverse * inverse * mean_cross
    if scales_ref is not None:
        for row, scales in enumerate((mean, slope, level, tilt)):
            scales_ref[row : row + 1, :] = scales

    def back(rows, inner):
        return total_ref[inner, :] * slope - level - (read(rows) - mean) * tilt

    return back


def own_lanes():
    block = lax.axis_index("height") // 2
    return pl.ds(pl.multiple_of(block * NARROW, NARROW), NARROW)


def narrow_back(total_ref, value_ref, scales_ref):
    lanes = own_lanes()
    mean, slope, level, tilt = (scales_ref[row : row + 1, lanes] for row in range(4))
    return total_ref[:, lanes] * slope - level - (value_ref[:, lanes] - mean) * tilt


def turn_kernel(grad_ref, mask_ref, weights_ref, total_ref, taps_ref, *, cols):
    begin_back(grad_ref, weights_ref.at[1], mask_ref, taps_ref, total_ref, cols)


def norm_rows(table_ref, which):
    picks = (2 * which, 2 * which + 1, 6 + which, 9 + which)
    return tuple(table_ref[pick : pick + 1, :] for pick in picks)


def build_masks(ids_ref, mask_ref, lanes_ref, id_rows_ref, id_cols_ref, cols):
    rows = ids_ref.shape[1]

    def one_row(row, carry):
        here = ids_ref[0, row]
        place = pl.ds(pl.multiple_of(row * cols, cols), cols)
        id_rows_ref[place, :] = jnp.full((cols, LANES), here, jnp.int32)
        for side, other in ((0, row - 1), (1, row + 1)):
            inside = jnp.logical_and(other >= 0, other < rows)
            other_id = ids_ref[0, jnp.clip(other, 0, rows - 1)]
            same = jnp.where(jnp.logical_and(inside, other_id == here), 1.0, 0.0)
            mask_ref[side, place, :] = jnp.full((cols, LANES), same, jnp.float32)
        return carry

    lax.fori_loop(0, rows, one_row, 0)
    lane = lax.broadcasted_iota(jnp.int32, (8, LANES), 1)
    each = LANES // cols
    for block in range(rows // each):
        ids = jnp.full((8, LANES), ids_ref[0, block * each], jnp.int32)
        for step in range(1, each):
            ids = jnp.where(lane >= step * cols, ids_ref[0, block * each + step], ids)
        id_cols_ref[:, block * LANES : (block + 1) * LANES] = ids
    ids = id_cols_ref[...].astype(jnp.float32)
    pixels = ids.shape[1]
    pixel = lax.broadcasted_iota(jnp.int32, ids.shape, 1)
    above = jnp.where(pixel < cols, -1.0, pltpu.roll(ids, cols, 1))
    below = jnp.where(pixel >= pixels - cols, -1.0, pltpu.roll(ids, pixels - cols, 1))
    lanes_ref[0:1, :] = jnp.where(above == ids, 1.0, 0.0)[0:1]
    lanes_ref[1:2, :] = jnp.where(below == ids, 1.0, 0.0)[0:1]


def place_pieces(pieces, whole_ref, sems):
    own_pixels = whole_ref.shape[0] // len(pieces)
    height = lax.axis_index("height")
    copies = []
    for place, piece in enumerate(pieces):
        piece = piece.at[piece.shape[0] - own_pixels : piece.shape[0], :]
        start = pl.multiple_of((height ^ place) * own_pixels, own_pixels)
        rows = pl.ds(start, own_pixels)
        copies.append(pltpu.make_async_copy(piece, whole_ref.at[rows, :], sems.at[place]))
    return copies


def hold_kernel(
    ids_hbm,
    gains_hbm,
    shifts_hbm,
    biases_hbm,
    weights_hbm,
    qkv_hbm,
    proj_hbm,
    qv_bias_hbm,
    proj_bias_hbm,
    weights_ref,
    turned_ref,
    qkv_ref,
    proj_ref,
    table_ref,
    mask_ref,
    lanes_ref,
    id_rows_ref,
    id_cols_ref,
    ids_ref,
    gains_ref,
    shifts_ref,
    biases_ref,
    qv_bias_ref,
    proj_bias_ref,
    sems,
    *,
    cols,
):
    channels = weights_ref.shape[-1]
    small = [
        (ids_hbm, ids_ref),
        (gains_hbm, gains_ref),
        (shifts_hbm, shifts_ref),
        (biases_hbm, biases_ref),
        (qv_bias_hbm, qv_bias_ref),
        (proj_bias_hbm, proj_bias_ref),
    ]
    large = [(weights_hbm, weights_ref), (qkv_hbm, qkv_ref), (proj_hbm, proj_ref)]
    for which in range(2):
        for row_tap in range(3):
            for col_tap in range(3):
                place = slice(col_tap * channels, (col_tap + 1) * channels)
                large.append(
                    (
                        weights_hbm.at[which, 2 - row_tap, 2 - col_tap],
                        turned_ref.at[which, row_tap, :, place],
                    )
                )
    copies = [
        pltpu.make_async_copy(source, target, sems.at[index])
        for index, (source, target) in enumerate(small + large)
    ]
    for copy in copies:
        copy.start()
    for copy in copies[: len(small)]:
        copy.wait()
    build_masks(ids_ref, mask_ref, lanes_ref, id_rows_ref, id_cols_ref, cols)
    table_ref[6:9, :] = gains_ref[...]
    table_ref[9:12, :] = shifts_ref[...]
    table_ref[12:14, :] = biases_ref[...]
    table_ref[14:16, :] = qv_bias_ref[...]
    table_ref[16:17, :] = proj_bias_ref[...]
    for copy in copies[len(small) :]:
        copy.wait()


def conv_kernel(*refs, cols, count):
    pieces, refs = refs[:count], refs[count:]
    (
        weights_ref,
        params_ref,
        mask_ref,
        features_ref,
        act_one_ref,
        middle_ref,
        act_two_ref,
        residual_ref,
        table_ref,
        own_ref,
        taps_ref,
        sem,
    ) = refs
    pixels, channels = features_ref.shape
    wide = jnp.float32
    own_copy = pltpu.make_async_copy(pieces[0], own_ref, sem)
    own_copy.start()
    table_ref[...] = params_ref[...]
    clear_edges(taps_ref, cols)

    def read_input(rows):
        return features_ref[rows, :].astype(wide)

    def read_middle(rows):
        return middle_ref[rows, :]

    height = lax.axis_index("height")
    own_pixels = pixels // count
    seen = RunningStats(channels)
    for place in list(range(1, count)) + [0]:
        if place == 0:
            own_copy.wait()
        piece = (pieces[place] if place else own_ref)[0:own_pixels, :]
        start = pl.multiple_of((height ^ place) * own_pixels, own_pixels)
        features_ref[pl.ds(start, own_pixels), :] = piece
        seen.add(piece.astype(wide))
    table_ref[0:1, :], table_ref[1:2, :] = seen.finish(pixels)
    seen = RunningStats(channels)

    def keep(rows, value):
        seen.add(value)
        return value

    run_conv(
        taps_ref,
        product_forward(weights_ref.at[0]),
        mask_ref,
        middle_ref,
        activation(read_input, *norm_rows(table_ref, 0), act_one_ref, taps_ref, cols),
        lambda rows, part: part + table_ref[12:13, :],
        keep,
        cols,
    )
    table_ref[2:3, :], table_ref[3:4, :] = seen.finish(pixels)
    seen = RunningStats(channels)
    run_conv(
        taps_ref,
        product_forward(weights_ref.at[1]),
        mask_ref,
        residual_ref,
        activation(read_middle, *norm_rows(table_ref, 1), act_two_ref, taps_ref, cols),
        lambda rows, part: part + (read_input(rows) + table_ref[13:14, :]),
        keep,
        cols,
    )
    table_ref[4:5, :], table_ref[5:6, :] = seen.finish(pixels)


def score_kernel(
    qkv_ref,
    proj_ref,
    residual_ref,
    table_ref,
    id_rows_ref,
    id_cols_ref,
    normed_ref,
    query_ref,
    key_ref,
    value_ref,
    soft_ref,
    out_flip_ref,
    output_ref,
    value_flip_ref,
    *scores_refs,
    score_scale,
):
    pixels, channels = residual_ref.shape
    own_pixels = output_ref.shape[0]
    wide = jnp.float32
    exponent = score_scale * 1.4426950408889634
    mean, inverse, gain, shift = norm_rows(table_ref, 2)
    scale = inverse * gain

    def normalise(start):
        rows = slice(start, start + KEY_ROWS)
        normed = (residual_ref[rows, :] - mean) * scale + shift
        normed_ref[rows, :] = normed.astype(jnp.bfloat16)

    def project(start):
        rows = slice(start, start + KEY_ROWS)
        normed = normed_ref[rows, :]
        query_ref[rows, :] = (
            jnp.dot(normed, qkv_ref[:, 0:channels], preferred_element_type=wide)
            + table_ref[14:15, :]
        ).astype(jnp.bfloat16)
        key_ref[rows, :] = jnp.dot(
            normed, qkv_ref[:, channels : 2 * channels], preferred_element_type=wide
        ).astype(jnp.bfloat16)
        values = (
            jnp.dot(normed, qkv_ref[:, 2 * channels :], preferred_element_type=wide)
            + table_ref[15:16, :]
        ).astype(jnp.bfloat16)
        value_ref[rows, :] = values
        value_flip_ref[:, rows] = values.T

    normalise(0)
    for start in range(0, pixels, KEY_ROWS):
        if start + KEY_ROWS < pixels:
            normalise(start + KEY_ROWS)
        project(start)
    block = scores_refs[0].shape[1]
    steps = range(0, pixels, KEY_ROWS)

    def score(index):
        rows = slice(index * block, (index + 1) * block)
        for start in steps:
            keys = slice(start, start + KEY_ROWS)
            scores = lax.dot_general(
                key_ref[keys, :],
                query_ref[rows, :],
                (((1,), (1,)), ((), ())),
                preferred_element_type=wide,
            )
            same = widen(id_rows_ref[keys, :], block) == id_cols_ref[0:1, rows]
            scores_refs[index][keys, :] = jnp.where(same, scores, masked_score)

    def soften(index):
        rows = slice(index * block, (index + 1) * block)
        scores_ref = scores_refs[index]
        peak = jnp.full((8, block), masked_score, wide)
        for start in steps:
            scores = scores_ref[start : start + KEY_ROWS, :]
            peak = jnp.maximum(peak, jnp.max(scores.reshape(-1, 8, block), axis=0))
        peak = jnp.max(peak, axis=0, keepdims=True)
        total = jnp.zeros((8, block), wide)
        for start in steps:
            keys = slice(start, start + KEY_ROWS)
            powers = jnp.exp2((scores_ref[keys, :] - peak) * exponent)
            scores_ref[keys, :] = powers
            total = total + fold(powers)
        share = 1.0 / column_total(total)
        for start in steps:
            keys = slice(start, start + KEY_ROWS)
            soft_ref[keys, rows] = (scores_ref[keys, :] * share).astype(jnp.bfloat16)

    score(0)
    for index in range(len(scores_refs)):
        if index + 1 < len(scores_refs):
            score(index + 1)
        soften(index)

    def collect(rows, carry):
        out_flip_ref[rows, :] = jnp.dot(
            value_flip_ref[rows, :], soft_ref[...], preferred_element_type=wide
        ).astype(jnp.bfloat16)
        return carry

    each_block(channels, channels // 2, collect)
    height = lax.axis_index("height")
    own = pl.ds(pl.multiple_of(height * own_pixels, own_pixels), own_pixels)
    output_ref[...] = (
        residual_ref[own, :]
        + lax.dot_general(
            out_flip_ref[:, own],
            proj_ref[...],
            (((0,), (0,)), ((), ())),
            preferred_element_type=wide,
        )
        + table_ref[16:17, :]
    ).astype(jnp.bfloat16)


def own_quarter():
    height = lax.axis_index("height")
    return (height & 1) * 2 + ((height >> 1) & 1)


def attention_kernel(
    proj_ref,
    normed_ref,
    query_ref,
    key_ref,
    value_ref,
    soft_ref,
    out_flip_ref,
    *refs,
    score_scale,
    count,
):
    pieces, (grad_ref, packed_ref, sums_ref), refs = (
        refs[:count],
        refs[count : count + 3],
        refs[count + 3 :],
    )
    pixels, channels = normed_ref.shape
    blocks = pixels // SCORE_ROWS
    grads_refs, refs = refs[-blocks:], refs[:-blocks]
    keep_ref, send_ref, mixed_ref, key_flip_ref, back_ref, score_grad_ref, flip_ref, sems = refs
    wide = jnp.float32
    copies = place_pieces(pieces, grad_ref, sems)
    for copy in copies:
        copy.start()
    quarter = channels // 4
    own = pl.ds(pl.multiple_of(own_quarter() * quarter, quarter), quarter)
    flip_ref[...] = normed_ref[:, own].T
    key_flip_ref[...] = key_ref[...].T
    for copy in copies:
        copy.wait()
    block, count = SCORE_ROWS, blocks
    steps = range(0, pixels, KEY_ROWS)

    def block_rows(index):
        return slice(index * block, (index + 1) * block)

    for index in range(count):
        back_ref[block_rows(index), :] = lax.dot_general(
            grad_ref[block_rows(index), :],
            proj_ref[...],
            (((1,), (1,)), ((), ())),
            preferred_element_type=wide,
        ).astype(jnp.bfloat16)

    def weigh(index):
        total = jnp.zeros((8, block), wide)
        for start in steps:
            keys = slice(start, start + KEY_ROWS)
            weight_grad = lax.dot_general(
                value_ref[keys, :],
                back_ref[block_rows(index), :],
                (((1,), (1,)), ((), ())),
                preferred_element_type=wide,
            )
            grads_refs[index][keys, :] = weight_grad
            total = total + fold(soft_ref[keys, block_rows(index)].astype(wide) * weight_grad)
        return column_total(total)

    def slope(index, dots):
        for start in steps:
            keys = slice(start, start + KEY_ROWS)
            weights = soft_ref[keys, block_rows(index)].astype(wide)
            score_grad_ref[keys, block_rows(index)] = (
                weights * (grads_refs[index][keys, :] - dots)
            ).astype(jnp.bfloat16)

    dots = weigh(0)
    for index in range(count):
        now, rows = dots, block_rows(index)
        if index + 1 < count:
            dots = weigh(index + 1)
        slope(index, now)
        packed_ref[rows, 2 * channels :] = jnp.dot(
            soft_ref[rows, :], back_ref[...], preferred_element_type=wide
        ).astype(jnp.bfloat16)
        query_grad = jnp.dot(
            key_flip_ref[...], score_grad_ref[:, rows], preferred_element_type=wide
        )
        packed_ref[rows, 0:channels] = (query_grad * score_scale).astype(jnp.bfloat16).T
    for index in range(count):
        rows = block_rows(index)
        packed_ref[rows, channels : 2 * channels] = (
            jnp.dot(score_grad_ref[rows, :], query_ref[...], preferred_element_type=wide)
            * score_scale
        ).astype(jnp.bfloat16)

    def pack(rows, carry):
        return (
            carry[0] + fold(packed_ref[rows, 0:channels].astype(wide)),
            carry[1] + fold(packed_ref[rows, 2 * channels :].astype(wide)),
            carry[2] + fold(grad_ref[rows, :].astype(wide)),
        )

    zeros = jnp.zeros((8, channels), wide)
    totals = zeros, zeros, zeros
    for start in range(0, pixels, CHUNK):
        totals = pack(pl.ds(start, CHUNK), totals)
    sums_ref[...] = jnp.zeros(sums_ref.shape, wide)
    for row, total in enumerate(totals):
        sums_ref[8 + row : 9 + row, :] = column_total(total)
    mixed_ref[:, 0 : 3 * channels] = jnp.dot(
        flip_ref[...], packed_ref[...], preferred_element_type=wide
    ).astype(jnp.bfloat16)
    mixed_ref[:, 3 * channels :] = jnp.dot(
        out_flip_ref[own, :], grad_ref[...], preferred_element_type=wide
    ).astype(jnp.bfloat16)
    keep_half(mixed_ref, 0, keep_ref, send_ref)


def third_kernel(
    qkv_ref,
    grad_ref,
    packed_ref,
    residual_ref,
    table_ref,
    act_two_ref,
    lanes_ref,
    old_sums_ref,
    residual_grad_ref,
    grad_two_ref,
    sums_ref,
    part_ref,
    total_ref,
    flip_ref,
    columns_ref,
    *,
    cols,
):
    pixels, channels = residual_ref.shape
    block = FILL_ROWS
    wide = jnp.float32
    mean, inverse, gain, shift = norm_rows(table_ref, 2)
    zeros = jnp.zeros((8, channels), wide)

    sums = (zeros, zeros)
    for start in range(0, pixels, block):
        rows = pl.ds(start, block)
        normed_grad = lax.dot_general(
            packed_ref[rows, :], qkv_ref[...], (((1,), (1,)), ((), ())), preferred_element_type=wide
        )
        total_ref[rows, :] = normed_grad
        centered = residual_ref[rows, :] - mean
        sums = sums[0] + fold(normed_grad), sums[1] + fold(normed_grad * centered)
    sums = sums[0], sums[1] * inverse
    sums_ref[...] = old_sums_ref[...]
    sums_ref[5:6, :] = column_total(sums[1])
    sums_ref[6:7, :] = column_total(sums[0])
    back = norm_back(
        total_ref, False, sums, lambda rows: residual_ref[rows, :], table_ref, 2, pixels
    )

    def finish(rows, carry):
        total = grad_ref[rows, :].astype(wide) + back(rows, rows)
        residual_grad_ref[rows, :] = total
        low = total.astype(jnp.bfloat16)
        grad_two_ref[rows, :] = low
        return carry + fold(low.astype(wide))

    sums_ref[7:8, :] = column_total(each_chunk(pixels, finish, zeros))
    narrow = grad_two_ref[:, own_lanes()]
    weight_part(act_two_ref, narrow, lanes_ref, flip_ref, columns_ref, part_ref, cols)


def second_kernel(
    old_total_ref,
    taps_ref,
    middle_ref,
    table_ref,
    act_one_ref,
    mask_ref,
    lanes_ref,
    weights_ref,
    old_sums_ref,
    part_two_ref,
    grad_one_ref,
    sums_ref,
    keep_one_ref,
    send_one_ref,
    keep_two_ref,
    send_two_ref,
    total_ref,
    flip_ref,
    columns_ref,
    part_ref,
    scales_ref,
    *,
    cols,
):
    pixels, channels = middle_ref.shape

    def read(rows):
        return middle_ref[rows, :]

    sums = finish_back(
        weights_ref.at[1], mask_ref, taps_ref, total_ref, read, table_ref, 1, cols, old_total_ref
    )
    back = norm_back(total_ref, True, sums, read, table_ref, 1, pixels, scales_ref)
    narrow = narrow_back(total_ref, middle_ref, scales_ref).astype(jnp.bfloat16)
    weight_part(act_one_ref, narrow, lanes_ref, flip_ref, columns_ref, part_ref, cols)
    sums_ref[...] = old_sums_ref[...]
    sums_ref[2:3, :] = column_total(sums[1])
    sums_ref[3:4, :] = column_total(sums[0])

    def finish(rows, carry):
        low = back(rows, rows).astype(jnp.bfloat16)
        grad_one_ref[rows, :] = low
        return carry + fold(low.astype(jnp.float32))

    zeros = jnp.zeros((8, channels), jnp.float32)
    sums_ref[4:5, :] = column_total(each_chunk(pixels, finish, zeros))
    keep_half(part_ref, 1, keep_one_ref, send_one_ref)
    keep_half(part_two_ref, 1, keep_two_ref, send_two_ref)


def near_far():
    core = lax.axis_index("height") & 1
    return 1 + core, 2 - core


def keep_half(source_ref, axis, keep_ref, send_ref):
    me = lax.axis_index("canvas")
    near, far = near_far()
    rows, width = keep_ref.shape[0] // 2, keep_ref.shape[1]
    for target_ref, flip in ((keep_ref, 0), (send_ref, near)):
        for slot, other in enumerate((0, far)):
            owner = me ^ flip ^ other
            target = target_ref.at[slot * rows : (slot + 1) * rows, :]
            if axis == 0:
                target[...] = source_ref[pl.ds(pl.multiple_of(owner * rows, rows), rows), :]
            else:
                target[...] = source_ref[:, pl.ds(pl.multiple_of(owner * width, width), width)]


def first_kernel(
    grad_one_ref,
    features_ref,
    table_ref,
    mask_ref,
    old_sums_ref,
    weights_ref,
    own_ref,
    sums_ref,
    partial_ref,
    total_ref,
    taps_ref,
    *,
    cols,
):
    def read(rows):
        return features_ref[rows, :].astype(jnp.float32)

    weights = weights_ref.at[0]
    begin_back(grad_one_ref, weights, mask_ref, taps_ref, total_ref, cols)
    sums = finish_back(weights, mask_ref, taps_ref, total_ref, read, table_ref, 0, cols)
    partial_ref[0:8, :], partial_ref[8:16, :] = sums
    sums_ref[...] = old_sums_ref[...]
    sums_ref[0:1, :] = column_total(sums[1])
    sums_ref[1:2, :] = column_total(sums[0])
    count = own_ref.shape[0]
    own = pl.ds(pl.multiple_of(lax.axis_index("height") * count, count), count)
    own_ref[...] = total_ref[own, :]


def own_kernel(
    own_ref, partial_ref, features_ref, residual_grad_ref, table_ref, input_grad_ref
):
    def read(rows):
        return features_ref[rows, :].astype(jnp.float32)

    sums = partial_ref[0:8, :], partial_ref[8:16, :]
    pixels = features_ref.shape[0]
    back = norm_back(own_ref, True, sums, read, table_ref, 0, pixels)
    count = own_ref.shape[0]
    own = pl.ds(pl.multiple_of(lax.axis_index("height") * count, count), count)
    total = residual_grad_ref[own, :] + back(own, slice(0, count))
    input_grad_ref[...] = total.astype(jnp.bfloat16)


def place_kernel(*refs):
    joints, packed_ref = refs[:-1], refs[-1]
    share = packed_ref.shape[0] // len(joints)
    me = lax.axis_index("canvas")
    for step, joint in enumerate(joints):
        place = pl.ds(pl.multiple_of((me ^ step) * share, share), share)
        packed_ref[place, :] = joint[...]


def cut_kernel(packed_ref, *half_refs):
    rows = half_refs[0].shape[0]
    for index, half_ref in enumerate(half_refs):
        half_ref[...] = packed_ref[index * rows : (index + 1) * rows, :]


def spread_quarters(packed, flips, qkv_ref, proj_ref, qkv_hbm, proj_hbm, sems):
    quarter = packed[0].shape[0]
    inner = qkv_ref.shape[2]
    copies = []
    for index, packed_ref in enumerate(packed):
        owner = own_quarter() ^ flips[index]
        rows = pl.ds(pl.multiple_of(owner * quarter, quarter), quarter)
        qkv_ref[index] = packed_ref[:, 0:inner].astype(jnp.float32)
        proj_ref[index] = packed_ref[:, inner:].astype(jnp.float32)
        for which, (held, target) in enumerate(((qkv_ref, qkv_hbm), (proj_ref, proj_hbm))):
            copy = pltpu.make_async_copy(held.at[index], target.at[rows, :], sems.at[index, which])
            copy.start()
            copies.append(copy)
    return copies


def join_kernel(*refs):
    packed, (qkv_hbm, proj_hbm, qkv_ref, proj_ref, sems) = refs[:-5], refs[-5:]
    copies = spread_quarters(packed, [0, 2], qkv_ref, proj_ref, qkv_hbm, proj_hbm, sems)
    for copy in copies:
        copy.wait()


def halve_kernel(keep_ref, got_ref, hold_ref, send_ref):
    total = keep_ref[...].astype(jnp.float32) + got_ref[...].astype(jnp.float32)
    rows = hold_ref.shape[0]
    hold_ref[...] = total[0:rows]
    send_ref[0:rows, :] = total[rows:].astype(jnp.bfloat16)


def halve_sums_kernel(
    keep_ref,
    got_ref,
    keep_two_ref,
    got_two_ref,
    sums_ref,
    got_sums_ref,
    hold_ref,
    send_ref,
    hold_two_ref,
    both_ref,
):
    rows = hold_ref.shape[0]
    halve_kernel(keep_ref, got_ref, hold_ref, send_ref)
    halve_kernel(keep_two_ref, got_two_ref, hold_two_ref, send_ref.at[rows : 2 * rows, :])
    rows *= 2
    left = sums_ref[...] + got_sums_ref[...]
    both_ref[...] = left
    count, width = left.shape
    for part in range(2):
        low = left.astype(jnp.bfloat16)
        left = left - low.astype(jnp.float32)
        for block in range(width // LANES):
            send_ref[rows : rows + count, :] = low[:, block * LANES : (block + 1) * LANES]
            rows += count


def unpack_sums(got_ref, rows, count, width):
    total = jnp.zeros((count, width), jnp.float32)
    for part in range(2):
        blocks = []
        for block in range(width // LANES):
            blocks.append(got_ref[rows : rows + count, :].astype(jnp.float32))
            rows += count
        total = total + jnp.concatenate(blocks, axis=1)
    return total


def last_kernel(
    chip_ref,
    both_a_ref,
    both_b_ref,
    old_qkv,
    old_proj,
    qkv_hbm,
    proj_hbm,
    qkv_ref,
    proj_ref,
    sems,
):
    copies = []
    rows = both_a_ref.shape[0]
    inner = qkv_ref.shape[2]
    chips = (chip_ref.at[0:rows, :], chip_ref.at[rows : 2 * rows, :])
    for index, piece_ref in enumerate((*chips, both_a_ref, both_b_ref)):
        start = ((own_quarter() ^ (1 if index < 2 else 3)) * 2 + index % 2) * rows
        target = pl.ds(pl.multiple_of(start, rows), rows)
        qkv_ref[index] = piece_ref[:, 0:inner].astype(jnp.float32)
        proj_ref[index] = piece_ref[:, inner:].astype(jnp.float32)
        for which, (held, whole) in enumerate(((qkv_ref, qkv_hbm), (proj_ref, proj_hbm))):
            copy = pltpu.make_async_copy(held.at[index], whole.at[target, :], sems.at[index, which])
            copy.start()
            copies.append(copy)
    for copy in copies:
        copy.wait()


def sums_kernel(
    sums_ref,
    hold_one_ref,
    hold_two_ref,
    got_ref,
    share_ref,
    gains_ref,
    shifts_ref,
    conv_ref,
    qv_ref,
    bias_ref,
):
    rows = hold_one_ref.shape[0]
    for which, hold_ref in enumerate((hold_one_ref, hold_two_ref)):
        got = got_ref[which * rows : (which + 1) * rows, :].astype(jnp.float32)
        share_ref[which] = (hold_ref[...] + got).reshape(share_ref.shape[1:])
    total = sums_ref[...]
    total = total + unpack_sums(got_ref, 2 * rows, *total.shape)
    for row, start in enumerate((0, 2, 5)):
        gains_ref[row : row + 1, :] = total[start : start + 1]
        shifts_ref[row : row + 1, :] = total[start + 1 : start + 2]
    conv_ref[0:1, :] = total[4:5]
    conv_ref[1:2, :] = total[7:8]
    qv_ref[...] = total[8:10]
    bias_ref[...] = total[10:11]


def call_kernel(kernel, outputs, scratch, operands, places, flops, limit, out_places=None, aliases={}):
    out_places = out_places or "v" * len(outputs)
    spaces = {
        "v": pl.BlockSpec(memory_space=pltpu.VMEM),
        "s": pl.BlockSpec(memory_space=pltpu.SMEM),
        "h": pl.BlockSpec(memory_space=pl.ANY),
        "o": pl.BlockSpec(memory_space=pltpu.VMEM),
        "a": pl.BlockSpec(memory_space=pl.ANY),
    }
    moved = 8 * flops // LANES
    held = {"v": pltpu.VMEM, "h": pltpu.HBM, "o": jax.ShapeDtypeStruct}
    operands = [
        pltpu.with_memory_space_constraint(array, pltpu.HBM) if place == "h" else array
        for array, place in zip(operands, places)
    ]
    return pl.pallas_call(
        kernel,
        out_shape=[held[place](*output) for output, place in zip(outputs, out_places)],
        in_specs=[spaces[place] for place in places],
        out_specs=[spaces[place] for place in out_places],
        scratch_shapes=scratch,
        input_output_aliases=aliases,
        compiler_params=pltpu.CompilerParams(vmem_limit_bytes=limit * 2**20),
        cost_estimate=pl.CostEstimate(flops=flops, bytes_accessed=moved, transcendentals=0),
    )(*operands)


def send_height(block, step):
    size = lax.axis_size("height")
    return lax.ppermute(block, "height", [(i, i ^ step) for i in range(size)])


def with_cores(blocks, other):
    pieces = [blocks[0], other]
    for block in blocks[1:]:
        pieces += [block, send_height(block, 1)]
    return pieces


def send_canvas(block, step):
    size = lax.axis_size("canvas")
    return lax.ppermute(block, "canvas", [(i, i ^ step) for i in range(size)])


def send_phase(block, phase):
    canvases, size = lax.axis_size("canvas"), lax.axis_size("height")
    pairs = []
    for canvas in range(canvases):
        for height in range(size):
            step = 2 if (height ^ phase) & 1 else 1
            pairs.append((canvas * size + height, (canvas ^ step) * size + height))
    return lax.ppermute(block, ("canvas", "height"), pairs)


def trade_canvas(pieces):
    return [pieces[0]] + [send_canvas(piece, step) for step, piece in enumerate(pieces) if step]


def whole_canvas(
    features,
    tile_ids,
    norm_gains,
    norm_shifts,
    conv_weights,
    conv_biases,
    qkv_weight,
    qv_bias,
    proj_weight,
    proj_bias,
    cotangent,
):
    height_size = lax.axis_size("height")
    canvas_size = lax.axis_size("canvas")
    local_rows, cols, channels = features.shape[1:]
    all_rows = tile_ids.shape[1]
    pixels = all_rows * cols
    own_pixels = local_rows * cols
    out_share = channels // height_size
    ci_share = channels // canvas_size
    quarter = channels // 4
    row_share = quarter // canvas_size
    low, wide = jnp.bfloat16, jnp.float32

    own_features = features.reshape(own_pixels, channels)
    own_grad = cotangent.reshape(own_pixels, channels)
    steps = range(2, height_size, 2)
    held_features = [own_features] + [send_height(own_features, step) for step in steps]
    plane = ((pixels, channels), low)
    plane_wide = ((pixels, channels), wide)
    sums_shape = ((16, channels), wide)
    mixed_halves = [((2 * row_share, 4 * channels), low)] * 2
    taps = pltpu.VMEM((pixels + 2 * cols, 3 * channels), low)
    held_wide = pltpu.VMEM((pixels, channels), wide)
    flipped = pltpu.VMEM((channels, pixels), low)
    narrow = pltpu.VMEM((NARROW, pixels), low)
    columns = pltpu.VMEM((9 * out_share, pixels), low)
    part_held = pltpu.VMEM((9 * out_share, channels), low)
    sem = pltpu.SemaphoreType.DMA
    conv_flops = 2 * 9 * pixels * channels * channels
    dot_flops = 2 * pixels * channels * channels
    score_flops = 2 * pixels * pixels * channels
    scale = channels ** (-0.5)

    (
        held_conv,
        turned,
        held_qkv,
        held_proj,
        params,
        mask,
        lane_mask,
        id_rows,
        id_cols,
    ) = call_kernel(
        functools.partial(hold_kernel, cols=cols),
        [
            (conv_weights.shape, low),
            ((2, 3, channels, 3 * channels), low),
            (qkv_weight.shape, low),
            (proj_weight.shape, low),
            ((24, channels), wide),
            ((2, pixels, LANES), wide),
            ((8, pixels), wide),
            ((pixels, LANES), jnp.int32),
            ((8, pixels), jnp.int32),
        ],
        [
            pltpu.SMEM(tile_ids.shape, jnp.int32),
            pltpu.VMEM(norm_gains.shape, wide),
            pltpu.VMEM(norm_shifts.shape, wide),
            pltpu.VMEM(conv_biases.shape, wide),
            pltpu.VMEM(qv_bias.shape, wide),
            pltpu.VMEM((1, channels), wide),
            sem((27,)),
        ],
        [
            tile_ids,
            norm_gains,
            norm_shifts,
            conv_biases,
            conv_weights,
            qkv_weight,
            proj_weight,
            qv_bias,
            proj_bias.reshape(1, channels),
        ],
        "h" * 9,
        conv_flops,
        8,
    )
    held_features[1:] = [
        lax.optimization_barrier((params, block))[1] for block in held_features[1:]
    ]
    params, first_features = lax.optimization_barrier((params, own_features))
    other_core = send_height(jnp.concatenate([first_features, own_grad], axis=0), 1)
    pieces = with_cores(held_features, other_core)
    far_grad, *pieces[4::2] = lax.optimization_barrier((own_grad, *held_features[2:]))
    held_grads = [own_grad, send_height(own_grad, 2)]
    held_grads[1], pieces[2] = lax.optimization_barrier((held_grads[1], held_features[1]))
    held_grads += [send_height(far_grad, step) for step in steps[1:]]

    all_features, act_one, middle, act_two, residual, table = call_kernel(
        functools.partial(conv_kernel, cols=cols, count=height_size),
        [plane, plane, plane_wide, plane, plane_wide, ((24, channels), wide)],
        [pltpu.VMEM((own_pixels, channels), low), taps, sem],
        [*pieces, held_conv, params, mask],
        "h" + "v" * (height_size + 2),
        2 * conv_flops,
        16,
    )
    residual, *held_grads = lax.optimization_barrier((residual, *held_grads))
    grad_pieces = with_cores(held_grads, other_core)
    normed, query, key, value, soft, out_flip, output = call_kernel(
        functools.partial(score_kernel, score_scale=scale),
        [
            plane,
            plane,
            plane,
            plane,
            ((pixels, pixels), low),
            ((channels, pixels), low),
            ((own_pixels, channels), low),
        ],
        [
            flipped,
            *[pltpu.VMEM((pixels, SCORE_ROWS), wide)] * (pixels // SCORE_ROWS),
        ],
        [
            held_qkv,
            held_proj,
            residual,
            table,
            id_rows,
            id_cols,
        ],
        "vvvvvv",
        3 * dot_flops + 2 * score_flops,
        20,
        "v" * 6 + "o",
    )
    normed, *grad_pieces = lax.optimization_barrier((normed, *grad_pieces))
    all_grad, packed, sums, keep_mixed, send_mixed = call_kernel(
        functools.partial(attention_kernel, score_scale=scale, count=height_size),
        [plane, ((pixels, 3 * channels), low), sums_shape, *mixed_halves],
        [
            pltpu.VMEM((quarter, 4 * channels), low),
            flipped,
            pltpu.VMEM((pixels, channels), low),
            pltpu.VMEM((pixels, pixels), low),
            pltpu.VMEM((quarter, pixels), low),
            sem((height_size,)),
            *[pltpu.VMEM((pixels, SCORE_ROWS), wide)] * (pixels // SCORE_ROWS),
        ],
        [held_proj, normed, query, key, value, soft, out_flip, *grad_pieces],
        "vvvvvvvh" + "a" * (height_size - 1),
        3 * dot_flops + 4 * score_flops,
        20,
    )
    got_mixed = send_phase(send_mixed, 0)
    residual_grad, grad_two, sums, part_two = call_kernel(
        functools.partial(third_kernel, cols=cols),
        [plane_wide, plane, sums_shape, ((9 * out_share, channels), low)],
        [held_wide, narrow, columns],
        [held_qkv, all_grad, packed, residual, table, act_two, lane_mask, sums],
        "vvvvvvvv",
        3 * dot_flops + conv_flops // height_size,
        16,
    )
    grad_two, got_mixed = lax.optimization_barrier((grad_two, got_mixed))
    hold_mixed, send_mixed = call_kernel(
        halve_kernel,
        [((row_share, 4 * channels), kind) for kind in (wide, low)],
        [],
        [keep_mixed, got_mixed],
        "vv",
        1,
        12,
    )
    got_mixed = send_phase(send_mixed, 1)
    grad_two, hold_mixed = lax.optimization_barrier((grad_two, hold_mixed))
    half_total, half_taps = call_kernel(
        functools.partial(turn_kernel, cols=cols),
        [plane_wide, (taps.shape, low)],
        [],
        [grad_two, mask, turned],
        "vvv",
        2 * conv_flops // 3,
        16,
    )
    half_total, got_mixed = lax.optimization_barrier((half_total, got_mixed))
    mixed_sum = (hold_mixed + got_mixed.astype(wide)).astype(low)
    joints = trade_canvas([mixed_sum] * canvas_size)
    halves = [((2 * 9 * out_share, ci_share), low)] * 4
    grad_one, sums, keep_one, send_one, keep_two, send_two = call_kernel(
        functools.partial(second_kernel, cols=cols),
        [plane, sums_shape, *halves],
        [held_wide, narrow, columns, part_held, pltpu.VMEM((8, channels), wide)],
        [half_total, half_taps, middle, table, act_one, mask, lane_mask, turned, sums, part_two],
        "v" * 10,
        conv_flops // 2,
        20,
    )
    grad_one, *joints = lax.optimization_barrier((grad_one, *joints))
    (own_mixed,) = call_kernel(
        place_kernel,
        [((quarter, 4 * channels), low)],
        [],
        joints,
        "v" * canvas_size,
        1,
        12,
    )
    own_mixed, send_one, send_two = lax.optimization_barrier((own_mixed, send_one, send_two))
    chip_mixed = send_height(own_mixed, 2)
    core_mixed = send_height(own_mixed, 1)
    got_one, got_two = send_phase(send_one, 0), send_phase(send_two, 0)
    own_total, sums, partial_sums = call_kernel(
        functools.partial(first_kernel, cols=cols),
        [((own_pixels, channels), wide), sums_shape, sums_shape],
        [held_wide, taps],
        [grad_one, all_features, table, mask, sums, turned],
        "vvvvvv",
        1,
        20,
    )
    got_sums = send_phase(sums, 0)
    (input_grad,) = call_kernel(
        own_kernel,
        [((own_pixels, channels), low)],
        [],
        [own_total, partial_sums, all_features, residual_grad, table],
        "vvvvv",
        dot_flops // 4,
        12,
        "o",
    )
    input_grad, got_sums, core_mixed, got_one, got_two = lax.optimization_barrier(
        (input_grad, got_sums, core_mixed, got_one, got_two)
    )
    share_rows = 9 * out_share
    send_rows = 2 * share_rows + 2 * sums_shape[0][0] * channels // LANES
    hold_one, send_share, hold_two, sums = call_kernel(
        halve_sums_kernel,
        [
            ((share_rows, ci_share), wide),
            ((send_rows, ci_share), low),
            ((share_rows, ci_share), wide),
            sums_shape,
        ],
        [],
        [keep_one, got_one, keep_two, got_two, sums, got_sums],
        "v" * 6,
        1,
        12,
    )
    got_share = send_phase(send_share, 1)

    def widened(count, rows):
        return [
            pltpu.VMEM((count, rows, 3 * channels), wide),
            pltpu.VMEM((count, rows, channels), wide),
            sem((count, 2)),
        ]

    grad_shapes = [(qkv_weight.shape, wide), (proj_weight.shape, wide)]
    core_mixed, hold_one = lax.optimization_barrier((core_mixed, hold_one))
    qkv_grad, proj_grad = call_kernel(
        join_kernel,
        grad_shapes,
        widened(2, quarter),
        [own_mixed, core_mixed],
        "vv",
        conv_flops,
        12,
        "hh",
    )
    qkv_grad, chip_mixed = lax.optimization_barrier((qkv_grad, chip_mixed))
    chip_halves = call_kernel(
        cut_kernel,
        [((quarter // 2, 4 * channels), low)] * 2,
        [],
        [chip_mixed],
        "v",
        1,
        12,
    )
    both_halves = [send_height(half, 1) for half in chip_halves]
    qkv_grad, proj_grad = call_kernel(
        last_kernel,
        grad_shapes,
        widened(4, quarter // 2),
        [chip_mixed, *both_halves, qkv_grad, proj_grad],
        "vvvhh",
        1,
        12,
        "hh",
        {3: 0, 4: 1},
    )
    qkv_grad, got_share = lax.optimization_barrier((qkv_grad, got_share))
    vector_shapes = [norm_gains.shape, norm_shifts.shape, conv_biases.shape, qv_bias.shape]
    conv_grad, gains_grad, shifts_grad, biases_grad, qv_grad, proj_bias_grad = call_kernel(
        sums_kernel,
        [((2, 3, 3, out_share, ci_share), wide)]
        + [(shape, wide) for shape in vector_shapes + [(1, channels)]],
        [],
        [sums, hold_one, hold_two, got_share],
        "vvvv",
        1,
        12,
        "o" * 6,
    )
    own_shape = (1, local_rows, cols, channels)
    return (
        output.reshape(own_shape),
        input_grad.reshape(own_shape),
        gains_grad,
        shifts_grad,
        jnp.swapaxes(conv_grad, 3, 4),
        biases_grad,
        qkv_grad,
        qv_grad,
        proj_grad,
        proj_bias_grad.reshape(channels),
    )


def on_device(*arrays):
    features, tile_ids = arrays[0], arrays[1]
    local_rows, cols, channels = features.shape[1:]
    pixels = tile_ids.shape[1] * cols
    height_size, canvas_size = lax.axis_size("height"), lax.axis_size("canvas")
    powers = all(size & (size - 1) == 0 for size in (height_size, canvas_size, cols))
    fits = (
        powers
        and height_size > 2
        and canvas_size == 4
        and channels == LANES * canvas_size
        and pixels <= MOST_PIXELS
        and pixels % FILL_ROWS == 0
        and FILL_ROWS % CHUNK == 0
        and pixels % SCORE_ROWS == 0
        and pixels % KEY_ROWS == 0
        and (local_rows * cols) % LANES == 0
        and CHUNK % cols == 0
        and cols % 16 == 0
        and channels % (LANES * canvas_size) == 0
        and 2 * channels == NARROW * height_size
    )
    return whole_canvas(*arrays) if fits else split_canvas(*arrays)


def solution(mesh):
    in_specs = (
        P("canvas", "height", None, None),
        P("canvas", None),
        P(),
        P(),
        P(),
        P(),
        P(),
        P(),
        P(),
        P(),
        P("canvas", "height", None, None),
    )
    out_specs = (
        P("canvas", "height", None, None),
        P("canvas", "height", None, None),
        P(),
        P(),
        P(None, None, None, "canvas", "height"),
        P(),
        P(),
        P(),
        P(),
        P(),
    )
    return jax.shard_map(
        on_device, mesh=mesh, in_specs=in_specs, out_specs=out_specs, check_vma=False
    )
```

```python
import functools

import jax
import jax.numpy as jnp
from jax import lax
from jax.experimental import pallas as pl
from jax.experimental.pallas import tpu as pltpu
from jax.sharding import PartitionSpec as P

GROUPS = 32


epsilon = 1e-06
masked_score = -1e30
MOST_PIXELS = 1024
LANES = 128
NARROW = 128
CHUNK = 128
FILL_ROWS = 256
QUERY_ROWS = 512
SCORE_ROWS = 256
KEY_ROWS = 256


def extended(block, sides, width):
    for axis, dim in sides:
        count = lax.axis_size(axis)
        forward = [(i, i + 1) for i in range(count - 1)]
        backward = [(target, source) for source, target in forward]
        low = lax.ppermute(
            lax.slice_in_dim(block, block.shape[dim] - width, None, axis=dim), axis, forward
        )
        high = lax.ppermute(lax.slice_in_dim(block, 0, width, axis=dim), axis, backward)
        block = jnp.concatenate([low, block, high], axis=dim)
    return block


def group_total(vector):
    return vector.reshape(GROUPS, -1).sum(axis=1)


def spread_groups(vector, channels):
    return jnp.repeat(vector, channels // GROUPS)


def norm_forward(values, gain, shift, members):
    channels = values.shape[1]
    totals = lax.psum(group_total(jnp.sum(values, axis=0)), "height")
    centered = values - spread_groups(totals / members, channels)
    squares = lax.psum(group_total(jnp.sum(centered * centered, axis=0)), "height")
    inverse = spread_groups(lax.rsqrt(squares / members + epsilon), channels)
    normed = centered * inverse
    return (normed, inverse, normed * gain + shift)


def norm_backward(grad_in, normed, inverse, gain, members):
    channels = grad_in.shape[1]
    scaled = grad_in * gain
    both_sums = lax.psum(
        (group_total(jnp.sum(scaled, axis=0)), group_total(jnp.sum(scaled * normed, axis=0))),
        "height",
    )
    mean_grad = spread_groups(both_sums[0] / members, channels)
    mean_cross = spread_groups(both_sums[1] / members, channels)
    result = inverse * (scaled - mean_grad - normed * mean_cross)
    return (result, jnp.sum(grad_in * normed, axis=0), jnp.sum(grad_in, axis=0))


def swish(values):
    return values * jax.nn.sigmoid(values)


def swish_slope(values):
    sigmoid_part = jax.nn.sigmoid(values)
    return sigmoid_part * (1.0 + values * (1.0 - sigmoid_part))


def tap_columns(padded, row_mask, local_rows, canvas_cols):
    pieces = []
    for row_tap in range(3):
        rows_taken = padded[row_tap : row_tap + local_rows] * row_mask[:, row_tap, None, None]
        for col_tap in range(3):
            pieces.append(rows_taken[:, col_tap : col_tap + canvas_cols])
    stacked = jnp.concatenate(pieces, axis=2)
    return stacked.reshape(local_rows * canvas_cols, stacked.shape[2])


def conv_forward(acts, row_mask, weight, bias):
    local_rows, canvas_cols, channels = acts.shape
    rimmed = extended(acts, (("height", 0),), 1)
    padded = jnp.pad(rimmed, ((0, 0), (1, 1), (0, 0)))
    gathered = tap_columns(padded, row_mask, local_rows, canvas_cols)
    result = (
        jnp.dot(
            gathered, weight.reshape(9 * channels, channels), preferred_element_type=jnp.float32
        )
        + bias
    )
    return (result, gathered)


def conv_backward(grad_low, row_mask, weight, gathered):
    local_rows, canvas_cols, channels = grad_low.shape
    flat_grad = grad_low.reshape(local_rows * canvas_cols, channels)
    weight_grad = lax.dot_general(
        gathered, flat_grad, (((0,), (0,)), ((), ())), preferred_element_type=jnp.float32
    )
    rimmed = extended(grad_low, (("height", 0),), 1)
    padded = jnp.pad(rimmed, ((0, 0), (1, 1), (0, 0)))
    grad_taps = tap_columns(padded, row_mask, local_rows, canvas_cols)
    flipped = jnp.transpose(weight[::-1, ::-1], (0, 1, 3, 2)).reshape(9 * channels, channels)
    input_part = jnp.dot(grad_taps, flipped, preferred_element_type=jnp.float32)
    return (
        input_part,
        weight_grad.reshape(3, 3, channels, channels),
        jnp.sum(flat_grad.astype(jnp.float32), axis=0),
    )


def take_rows(array, offset, count):
    return lax.dynamic_slice_in_dim(array, offset, count)


def score_grads(
    queries, out_grad, log_total, row_dots, query_ids, key_rows, value_rows, key_ids, score_scale
):
    scores = (
        lax.dot_general(
            queries, key_rows, (((1,), (1,)), ((), ())), preferred_element_type=jnp.float32
        )
        * score_scale
    )
    same_tile = query_ids[:, None] == key_ids[None, :]
    softmax_block = jnp.exp(jnp.where(same_tile, scores - log_total[:, None], masked_score))
    weight_grad = lax.dot_general(
        out_grad, value_rows, (((1,), (1,)), ((), ())), preferred_element_type=jnp.float32
    )
    score_grad = (softmax_block * (weight_grad - row_dots[:, None])).astype(jnp.bfloat16)
    return (softmax_block.astype(jnp.bfloat16), score_grad)


def split_canvas(
    features,
    tile_ids,
    norm_gains,
    norm_shifts,
    conv_weights,
    conv_biases,
    qkv_weight,
    qv_bias,
    proj_weight,
    proj_bias,
    cotangent,
):
    height_size = lax.axis_size("height")
    local_rows = features.shape[1]
    canvas_cols = features.shape[2]
    channels = features.shape[3]
    pixels = local_rows * canvas_cols
    row_ids = tile_ids[0]
    all_rows = row_ids.shape[0]
    members = float(all_rows * canvas_cols * (channels // GROUPS))
    score_scale = channels ** (-0.5)
    first_row = lax.axis_index("height") * local_rows
    edge_ids = jnp.full((1,), -1, jnp.int32)
    padded_ids = jnp.concatenate([edge_ids, row_ids, edge_ids])
    near_ids = lax.dynamic_slice_in_dim(padded_ids, first_row, local_rows + 2)
    own_rows = near_ids[1 : local_rows + 1]
    row_mask = jnp.stack(
        [near_ids[row_tap : row_tap + local_rows] == own_rows for row_tap in range(3)], axis=1
    ).astype(jnp.bfloat16)
    key_ids = jnp.repeat(row_ids, canvas_cols)
    query_ids = jnp.repeat(own_rows, canvas_cols)
    grid_shape = (local_rows, canvas_cols, channels)
    inputs = features[0].reshape(pixels, channels).astype(jnp.float32)
    normed_one, inverse_one, pre_one = norm_forward(inputs, norm_gains[0], norm_shifts[0], members)
    act_one = swish(pre_one).astype(jnp.bfloat16).reshape(grid_shape)
    middle, taps_one = conv_forward(act_one, row_mask, conv_weights[0], conv_biases[0])
    normed_two, inverse_two, pre_two = norm_forward(middle, norm_gains[1], norm_shifts[1], members)
    act_two = swish(pre_two).astype(jnp.bfloat16).reshape(grid_shape)
    branch, taps_two = conv_forward(act_two, row_mask, conv_weights[1], conv_biases[1])
    residual = inputs + branch
    normed_three, inverse_three, pre_three = norm_forward(
        residual, norm_gains[2], norm_shifts[2], members
    )
    attn_input = pre_three.astype(jnp.bfloat16)
    mixed = jnp.dot(attn_input, qkv_weight, preferred_element_type=jnp.float32)
    queries = (mixed[:, :channels] + qv_bias[0]).astype(jnp.bfloat16)
    key_rows = mixed[:, channels : 2 * channels].astype(jnp.bfloat16)
    value_rows = (mixed[:, 2 * channels :] + qv_bias[1]).astype(jnp.bfloat16)
    running_max = jnp.full((pixels,), masked_score, jnp.float32)
    key_piece = lax.all_gather(key_rows, "height", axis=0, tiled=True)
    value_piece = lax.all_gather(value_rows, "height", axis=0, tiled=True)
    scores = (
        lax.dot_general(
            queries, key_piece, (((1,), (1,)), ((), ())), preferred_element_type=jnp.float32
        )
        * score_scale
    )
    same_tile = query_ids[:, None] == key_ids[None, :]
    scores = jnp.where(same_tile, scores, masked_score)
    new_max = jnp.maximum(running_max, jnp.max(scores, axis=1))
    weights = jnp.where(same_tile, jnp.exp(scores - new_max[:, None]), 0.0)
    summed_out = jnp.dot(
        weights.astype(jnp.bfloat16), value_piece, preferred_element_type=jnp.float32
    )
    total_weight = jnp.sum(weights, axis=1)
    log_total = new_max + jnp.log(total_weight)
    attended = summed_out / total_weight[:, None]
    attended_low = attended.astype(jnp.bfloat16)
    output = (
        residual
        + jnp.dot(attended_low, proj_weight, preferred_element_type=jnp.float32)
        + proj_bias
    )
    out_grad = cotangent[0].reshape(pixels, channels)
    out_grad_full = out_grad.astype(jnp.float32)
    proj_grad = lax.dot_general(
        attended_low, out_grad, (((0,), (0,)), ((), ())), preferred_element_type=jnp.float32
    )
    proj_bias_grad = jnp.sum(out_grad_full, axis=0)
    attended_grad = lax.dot_general(
        out_grad, proj_weight, (((1,), (1,)), ((), ())), preferred_element_type=jnp.float32
    ).astype(jnp.bfloat16)
    row_dots = jnp.sum(attended_grad.astype(jnp.float32) * attended, axis=1)
    block_rows = pixels * min(height_size, 8)
    zero_block = jnp.zeros((pixels, channels), jnp.float32)
    key_all, value_all = (
        lax.all_gather(key_rows, "height", axis=0, tiled=True),
        lax.all_gather(value_rows, "height", axis=0, tiled=True),
    )
    query_all, grad_all = (
        lax.all_gather(queries, "height", axis=0, tiled=True),
        lax.all_gather(attended_grad, "height", axis=0, tiled=True),
    )
    total_all, dots_all = (
        lax.all_gather(log_total, "height", axis=0, tiled=True),
        lax.all_gather(row_dots, "height", axis=0, tiled=True),
    )

    def own_query_step(running, block_index):
        offset = block_index * block_rows
        key_part = take_rows(key_all, offset, block_rows)
        rounded, score_grad = score_grads(
            queries,
            attended_grad,
            log_total,
            row_dots,
            query_ids,
            key_part,
            take_rows(value_all, offset, block_rows),
            take_rows(key_ids, offset, block_rows),
            score_scale,
        )
        return (
            running
            + jnp.dot(score_grad, key_part, preferred_element_type=jnp.float32) * score_scale,
            None,
        )

    def own_key_step(running, block_index):
        offset = block_index * block_rows
        query_part = take_rows(query_all, offset, block_rows)
        grad_part = take_rows(grad_all, offset, block_rows)
        rounded, score_grad = score_grads(
            query_part,
            grad_part,
            take_rows(total_all, offset, block_rows),
            take_rows(dots_all, offset, block_rows),
            take_rows(key_ids, offset, block_rows),
            key_rows,
            value_rows,
            query_ids,
            score_scale,
        )
        key_part = (
            lax.dot_general(
                score_grad, query_part, (((0,), (0,)), ((), ())), preferred_element_type=jnp.float32
            )
            * score_scale
        )
        value_part = lax.dot_general(
            rounded, grad_part, (((0,), (0,)), ((), ())), preferred_element_type=jnp.float32
        )
        return ((running[0] + key_part, running[1] + value_part), None)

    block_count = key_all.shape[0] // block_rows
    query_grad, unused_one = lax.scan(own_query_step, zero_block, jnp.arange(block_count))
    (key_grad, value_grad), unused_two = lax.scan(
        own_key_step, (zero_block, zero_block), jnp.arange(block_count)
    )
    query_low = query_grad.astype(jnp.bfloat16)
    key_low = key_grad.astype(jnp.bfloat16)
    value_low = value_grad.astype(jnp.bfloat16)
    stacked_grad = jnp.concatenate([query_low, key_low, value_low], axis=1)
    qkv_grad = lax.dot_general(
        attn_input, stacked_grad, (((0,), (0,)), ((), ())), preferred_element_type=jnp.float32
    )
    qv_grad = jnp.stack(
        [
            jnp.sum(query_low.astype(jnp.float32), axis=0),
            jnp.sum(value_low.astype(jnp.float32), axis=0),
        ]
    )
    normed_grad = lax.dot_general(
        stacked_grad, qkv_weight, (((1,), (1,)), ((), ())), preferred_element_type=jnp.float32
    )
    back_three, gain_three, shift_three = norm_backward(
        normed_grad, normed_three, inverse_three, norm_gains[2], members
    )
    residual_grad = out_grad_full + back_three
    grad_two = residual_grad.astype(jnp.bfloat16).reshape(grid_shape)
    act_two_grad, weight_two_grad, bias_two_grad = conv_backward(
        grad_two, row_mask, conv_weights[1], taps_two
    )
    middle_grad, gain_two, shift_two = norm_backward(
        act_two_grad * swish_slope(pre_two), normed_two, inverse_two, norm_gains[1], members
    )
    grad_one = middle_grad.astype(jnp.bfloat16).reshape(grid_shape)
    act_one_grad, weight_one_grad, bias_one_grad = conv_backward(
        grad_one, row_mask, conv_weights[0], taps_one
    )
    input_back, gain_one, shift_one = norm_backward(
        act_one_grad * swish_slope(pre_one), normed_one, inverse_one, norm_gains[0], members
    )
    input_grad = residual_grad + input_back
    conv_grad = jnp.stack([weight_one_grad, weight_two_grad])
    conv_part = lax.psum_scatter(conv_grad, "height", scatter_dimension=4, tiled=True)
    conv_part = lax.psum_scatter(
        conv_part.astype(jnp.bfloat16), "canvas", scatter_dimension=3, tiled=True
    ).astype(jnp.float32)
    summed = lax.psum(
        (
            jnp.stack([gain_one, gain_two, gain_three]),
            jnp.stack([shift_one, shift_two, shift_three]),
            jnp.stack([bias_one_grad, bias_two_grad]),
            qkv_grad,
            qv_grad,
            proj_grad,
            proj_bias_grad,
        ),
        ("canvas", "height"),
    )
    return (
        output.astype(jnp.bfloat16).reshape((1,) + grid_shape),
        input_grad.astype(jnp.bfloat16).reshape((1,) + grid_shape),
        summed[0],
        summed[1],
        conv_part,
        summed[2],
        summed[3],
        summed[4],
        summed[5],
        summed[6],
    )


def fold(block):
    rows, width = block.shape
    return jnp.sum(block.reshape(rows // 8, 8, width), axis=0)


def group_lanes(block, group):
    lane = lax.broadcasted_iota(jnp.int32, block.shape, 1)
    width = block.shape[1]
    step = 1
    while step < group:
        above = pltpu.roll(block, step, 1)
        below = pltpu.roll(block, width - step, 1)
        block = block + jnp.where((lane & step) != 0, above, below)
        step *= 2
    return block


def group_mean(partial, members):
    spread = group_lanes(partial, partial.shape[1] // GROUPS)
    return jnp.sum(spread, axis=0, keepdims=True) * (1.0 / members)


def widen(block, width):
    return jnp.concatenate([block] * (width // block.shape[1]), axis=1)


def each_block(pixels, block, body, carry=0):
    def step(index, carry):
        return body(pl.ds(pl.multiple_of(index * block, block), block), carry)

    return lax.fori_loop(0, pixels // block, step, carry)


def each_chunk(pixels, body, carry):
    return each_block(pixels, CHUNK, body, carry)


def aligned(start, step):
    return start if isinstance(start, int) else pl.multiple_of(start, step)


class RunningStats:
    def __init__(self, channels):
        self.width = channels // GROUPS
        self.reference = None
        self.sums = self.squares = jnp.zeros((8, channels), jnp.float32)

    def add(self, block):
        if self.reference is None:
            self.reference = group_mean(block[0:8], 8.0 * self.width)
        offset = block - self.reference
        self.sums = self.sums + fold(offset)
        self.squares = self.squares + fold(offset * offset)

    def finish(self, pixels):
        both = group_lanes(jnp.concatenate([self.sums, self.squares], axis=0), self.width)
        share = 1.0 / (pixels * self.width)
        offset = column_total(both[0:8]) * share
        variance = column_total(both[8:16]) * share - offset * offset
        return self.reference + offset, lax.rsqrt(jnp.maximum(variance, 0.0) + epsilon)


def put_taps(taps_ref, block, rows, cols):
    count, channels = block.shape
    place = lax.broadcasted_iota(jnp.int32, block.shape, 0) & (cols - 1)
    left = jnp.where(place == 0, 0.0, pltpu.roll(block, 1, 0))
    right = jnp.where(place == cols - 1, 0.0, pltpu.roll(block, count - 1, 0))
    inner = pl.ds(aligned(rows.start + cols, cols), count)
    taps_ref[inner, 0:channels] = left.astype(jnp.bfloat16)
    taps_ref[inner, channels : 2 * channels] = block.astype(jnp.bfloat16)
    taps_ref[inner, 2 * channels :] = right.astype(jnp.bfloat16)


def clear_edges(taps_ref, cols):
    edge = jnp.zeros((cols, taps_ref.shape[1]), taps_ref.dtype)
    taps_ref[0:cols, :] = edge
    taps_ref[taps_ref.shape[0] - cols :, :] = edge


def begin_conv(taps_ref, product, total_ref, fill, first, cols):
    for start in range(0, total_ref.shape[0], FILL_ROWS):
        for inner in range(start, start + FILL_ROWS, CHUNK):
            fill(pl.ds(inner, CHUNK))
        rows = pl.ds(start, FILL_ROWS)
        total_ref[rows, :] = first(rows, product(taps_ref, pl.ds(start + cols, FILL_ROWS), 1))


def add_rows(taps_ref, product, mask_ref, total_ref, row_tap, last, cols, old_ref=None):
    pixels, channels = total_ref.shape
    old_ref = total_ref if old_ref is None else old_ref

    def step(rows, shifted):
        part = product(taps_ref, shifted, row_tap)
        mask = widen(mask_ref[row_tap // 2, rows, :], channels)
        value = old_ref[rows, :] + mask * part
        total_ref[rows, :] = value if last is None else last(rows, value)

    block = 2 * FILL_ROWS if last is None else FILL_ROWS
    for start in range(0, pixels, block):
        step(pl.ds(start, block), pl.ds(start + row_tap * cols, block))


def run_conv(taps_ref, product, mask_ref, total_ref, fill, first, last, cols):
    begin_conv(taps_ref, product, total_ref, fill, first, cols)
    add_rows(taps_ref, product, mask_ref, total_ref, 0, None, cols)
    add_rows(taps_ref, product, mask_ref, total_ref, 2, last, cols)


def product_forward(weight_ref):
    channels = weight_ref.shape[-1]

    def product(taps_ref, shifted, row_tap):
        return jnp.dot(
            taps_ref[shifted, :],
            weight_ref[row_tap].reshape(3 * channels, channels),
            preferred_element_type=jnp.float32,
        )

    return product


def product_backward(weight_ref):
    def product(taps_ref, shifted, row_tap):
        return lax.dot_general(
            taps_ref[shifted, :],
            weight_ref[row_tap],
            (((1,), (1,)), ((), ())),
            preferred_element_type=jnp.float32,
        )

    return product


def activation(read, mean, inverse, gain, shift, act_ref, taps_ref, cols):
    scale, offset = 0.5 * inverse * gain, 0.5 * shift

    def fill(rows):
        half = (read(rows) - mean) * scale + offset
        act = half * (1.0 + jnp.tanh(half))
        act_ref[rows, :] = act.astype(jnp.bfloat16)
        put_taps(taps_ref, act, rows, cols)

    return fill


def back_means(sums, gain, pixels):
    channels = gain.shape[1]
    members = float(pixels * (channels // GROUPS))
    return group_mean(sums[0] * gain, members), group_mean(sums[1] * gain, members)


def column_total(partial):
    return jnp.sum(partial, axis=0, keepdims=True)


def weight_part(act_ref, narrow, lanes_ref, flip_ref, columns_ref, part_ref, cols):
    pixels, channels = act_ref.shape
    height = lax.axis_index("height")
    share = NARROW // 2
    flip_ref[...] = narrow.T
    own = pl.ds(pl.multiple_of((height % 2) * share, share), share)
    grad = flip_ref[own, :].astype(jnp.float32)
    column = lax.broadcasted_iota(jnp.int32, grad.shape, 1) & (cols - 1)
    for col_tap in range(3):
        shifted = grad
        if col_tap == 0:
            shifted = jnp.where(column == cols - 1, 0.0, pltpu.roll(grad, pixels - 1, 1))
        elif col_tap == 2:
            shifted = jnp.where(column == 0, 0.0, pltpu.roll(grad, 1, 1))
        for row_tap in range(3):
            tap = 3 * row_tap + col_tap
            place = slice(tap * share, (tap + 1) * share)
            if row_tap == 1:
                columns_ref[place, :] = shifted.astype(jnp.bfloat16)
                continue
            side, turn = (0, pixels - cols) if row_tap == 0 else (1, cols)
            masked = (shifted * lanes_ref[side : side + 1, :]).astype(jnp.bfloat16)
            columns_ref[place, :] = pltpu.roll(masked, turn, 1)
    part_ref[...] = jnp.dot(
        columns_ref[...], act_ref[...], preferred_element_type=jnp.float32
    ).astype(jnp.bfloat16)


def begin_back(grad_ref, weights_ref, mask_ref, taps_ref, total_ref, cols):
    clear_edges(taps_ref, cols)

    def fill(rows):
        put_taps(taps_ref, grad_ref[rows, :].astype(jnp.float32), rows, cols)

    product = product_backward(weights_ref)
    begin_conv(taps_ref, product, total_ref, fill, lambda rows, part: part, cols)
    add_rows(taps_ref, product, mask_ref, total_ref, 0, None, cols)


def finish_back(
    weights_ref, mask_ref, taps_ref, total_ref, read, table_ref, which, cols, old_ref=None
):
    mean, inverse, gain, shift = norm_rows(table_ref, which)
    scale, offset = 0.5 * inverse * gain, 0.5 * shift
    sums = []

    def slope(rows, value):
        centered = read(rows) - mean
        half = centered * scale + offset
        turn = jnp.tanh(half)
        double = value * ((1.0 + turn) * (1.0 + half * (1.0 - turn)))
        sums.append((fold(double), fold(double * centered)))
        return double

    add_rows(
        taps_ref, product_backward(weights_ref), mask_ref, total_ref, 2, slope, cols, old_ref
    )
    plain, cross = sum(pair[0] for pair in sums), sum(pair[1] for pair in sums)
    return 0.5 * plain, 0.5 * inverse * cross


def norm_back(total_ref, double, sums, read, table_ref, which, pixels, scales_ref=None):
    mean, inverse, gain, shift = norm_rows(table_ref, which)
    mean_grad, mean_cross = back_means(sums, gain, pixels)
    slope = inverse * gain * (0.5 if double else 1.0)
    level, tilt = inverse * mean_grad, inverse * inverse * mean_cross
    if scales_ref is not None:
        for row, scales in enumerate((mean, slope, level, tilt)):
            scales_ref[row : row + 1, :] = scales

    def back(rows, inner):
        return total_ref[inner, :] * slope - level - (read(rows) - mean) * tilt

    return back


def own_lanes():
    block = lax.axis_index("height") // 2
    return pl.ds(pl.multiple_of(block * NARROW, NARROW), NARROW)


def narrow_back(total_ref, value_ref, scales_ref):
    lanes = own_lanes()
    mean, slope, level, tilt = (scales_ref[row : row + 1, lanes] for row in range(4))
    return total_ref[:, lanes] * slope - level - (value_ref[:, lanes] - mean) * tilt


def turn_kernel(grad_ref, mask_ref, weights_ref, total_ref, taps_ref, *, cols):
    begin_back(grad_ref, weights_ref.at[1], mask_ref, taps_ref, total_ref, cols)


def norm_rows(table_ref, which):
    picks = (2 * which, 2 * which + 1, 6 + which, 9 + which)
    return tuple(table_ref[pick : pick + 1, :] for pick in picks)


def build_masks(ids_ref, mask_ref, lanes_ref, id_rows_ref, id_cols_ref, cols):
    rows = ids_ref.shape[1]

    def one_row(row, carry):
        here = ids_ref[0, row]
        place = pl.ds(pl.multiple_of(row * cols, cols), cols)
        id_rows_ref[place, :] = jnp.full((cols, LANES), here, jnp.int32)
        for side, other in ((0, row - 1), (1, row + 1)):
            inside = jnp.logical_and(other >= 0, other < rows)
            other_id = ids_ref[0, jnp.clip(other, 0, rows - 1)]
            same = jnp.where(jnp.logical_and(inside, other_id == here), 1.0, 0.0)
            mask_ref[side, place, :] = jnp.full((cols, LANES), same, jnp.float32)
        return carry

    lax.fori_loop(0, rows, one_row, 0)
    lane = lax.broadcasted_iota(jnp.int32, (8, LANES), 1)
    each = LANES // cols
    for block in range(rows // each):
        ids = jnp.full((8, LANES), ids_ref[0, block * each], jnp.int32)
        for step in range(1, each):
            ids = jnp.where(lane >= step * cols, ids_ref[0, block * each + step], ids)
        id_cols_ref[:, block * LANES : (block + 1) * LANES] = ids
    ids = id_cols_ref[...].astype(jnp.float32)
    pixels = ids.shape[1]
    pixel = lax.broadcasted_iota(jnp.int32, ids.shape, 1)
    above = jnp.where(pixel < cols, -1.0, pltpu.roll(ids, cols, 1))
    below = jnp.where(pixel >= pixels - cols, -1.0, pltpu.roll(ids, pixels - cols, 1))
    lanes_ref[0:1, :] = jnp.where(above == ids, 1.0, 0.0)[0:1]
    lanes_ref[1:2, :] = jnp.where(below == ids, 1.0, 0.0)[0:1]


def place_pieces(pieces, whole_ref, sems):
    own_pixels = whole_ref.shape[0] // len(pieces)
    height = lax.axis_index("height")
    copies = []
    for place, piece in enumerate(pieces):
        piece = piece.at[piece.shape[0] - own_pixels : piece.shape[0], :]
        start = pl.multiple_of((height ^ place) * own_pixels, own_pixels)
        rows = pl.ds(start, own_pixels)
        copies.append(pltpu.make_async_copy(piece, whole_ref.at[rows, :], sems.at[place]))
    return copies


def hold_kernel(
    ids_hbm,
    gains_hbm,
    shifts_hbm,
    biases_hbm,
    weights_hbm,
    qkv_hbm,
    proj_hbm,
    qv_bias_hbm,
    proj_bias_hbm,
    weights_ref,
    turned_ref,
    qkv_ref,
    proj_ref,
    table_ref,
    mask_ref,
    lanes_ref,
    id_rows_ref,
    id_cols_ref,
    ids_ref,
    gains_ref,
    shifts_ref,
    biases_ref,
    qv_bias_ref,
    proj_bias_ref,
    sems,
    *,
    cols,
):
    channels = weights_ref.shape[-1]
    small = [
        (ids_hbm, ids_ref),
        (gains_hbm, gains_ref),
        (shifts_hbm, shifts_ref),
        (biases_hbm, biases_ref),
        (qv_bias_hbm, qv_bias_ref),
        (proj_bias_hbm, proj_bias_ref),
    ]
    large = [(weights_hbm, weights_ref), (qkv_hbm, qkv_ref), (proj_hbm, proj_ref)]
    for which in range(2):
        for row_tap in range(3):
            for col_tap in range(3):
                place = slice(col_tap * channels, (col_tap + 1) * channels)
                large.append(
                    (
                        weights_hbm.at[which, 2 - row_tap, 2 - col_tap],
                        turned_ref.at[which, row_tap, :, place],
                    )
                )
    copies = [
        pltpu.make_async_copy(source, target, sems.at[index])
        for index, (source, target) in enumerate(small + large)
    ]
    for copy in copies:
        copy.start()
    for copy in copies[: len(small)]:
        copy.wait()
    build_masks(ids_ref, mask_ref, lanes_ref, id_rows_ref, id_cols_ref, cols)
    table_ref[6:9, :] = gains_ref[...]
    table_ref[9:12, :] = shifts_ref[...]
    table_ref[12:14, :] = biases_ref[...]
    table_ref[14:16, :] = qv_bias_ref[...]
    table_ref[16:17, :] = proj_bias_ref[...]
    for copy in copies[len(small) :]:
        copy.wait()


def conv_kernel(*refs, cols, count):
    pieces, refs = refs[:count], refs[count:]
    (
        weights_ref,
        params_ref,
        mask_ref,
        features_ref,
        act_one_ref,
        middle_ref,
        act_two_ref,
        residual_ref,
        table_ref,
        own_ref,
        taps_ref,
        sem,
    ) = refs
    pixels, channels = features_ref.shape
    wide = jnp.float32
    own_copy = pltpu.make_async_copy(pieces[0], own_ref, sem)
    own_copy.start()
    table_ref[...] = params_ref[...]
    clear_edges(taps_ref, cols)

    def read_input(rows):
        return features_ref[rows, :].astype(wide)

    def read_middle(rows):
        return middle_ref[rows, :]

    height = lax.axis_index("height")
    own_pixels = pixels // count
    seen = RunningStats(channels)
    for place in list(range(1, count)) + [0]:
        if place == 0:
            own_copy.wait()
        piece = (pieces[place] if place else own_ref)[0:own_pixels, :]
        start = pl.multiple_of((height ^ place) * own_pixels, own_pixels)
        features_ref[pl.ds(start, own_pixels), :] = piece
        seen.add(piece.astype(wide))
    table_ref[0:1, :], table_ref[1:2, :] = seen.finish(pixels)
    seen = RunningStats(channels)

    def keep(rows, value):
        seen.add(value)
        return value

    run_conv(
        taps_ref,
        product_forward(weights_ref.at[0]),
        mask_ref,
        middle_ref,
        activation(read_input, *norm_rows(table_ref, 0), act_one_ref, taps_ref, cols),
        lambda rows, part: part + table_ref[12:13, :],
        keep,
        cols,
    )
    table_ref[2:3, :], table_ref[3:4, :] = seen.finish(pixels)
    seen = RunningStats(channels)
    run_conv(
        taps_ref,
        product_forward(weights_ref.at[1]),
        mask_ref,
        residual_ref,
        activation(read_middle, *norm_rows(table_ref, 1), act_two_ref, taps_ref, cols),
        lambda rows, part: part + (read_input(rows) + table_ref[13:14, :]),
        keep,
        cols,
    )
    table_ref[4:5, :], table_ref[5:6, :] = seen.finish(pixels)


def score_kernel(
    qkv_ref,
    proj_ref,
    residual_ref,
    table_ref,
    id_rows_ref,
    id_cols_ref,
    normed_ref,
    query_ref,
    key_ref,
    value_ref,
    soft_ref,
    out_flip_ref,
    output_ref,
    value_flip_ref,
    *scores_refs,
    score_scale,
):
    pixels, channels = residual_ref.shape
    own_pixels = output_ref.shape[0]
    wide = jnp.float32
    exponent = score_scale * 1.4426950408889634
    mean, inverse, gain, shift = norm_rows(table_ref, 2)
    scale = inverse * gain

    def normalise(start):
        rows = slice(start, start + KEY_ROWS)
        normed = (residual_ref[rows, :] - mean) * scale + shift
        normed_ref[rows, :] = normed.astype(jnp.bfloat16)

    def project(start):
        rows = slice(start, start + KEY_ROWS)
        normed = normed_ref[rows, :]
        query_ref[rows, :] = (
            jnp.dot(normed, qkv_ref[:, 0:channels], preferred_element_type=wide)
            + table_ref[14:15, :]
        ).astype(jnp.bfloat16)
        key_ref[rows, :] = jnp.dot(
            normed, qkv_ref[:, channels : 2 * channels], preferred_element_type=wide
        ).astype(jnp.bfloat16)
        values = (
            jnp.dot(normed, qkv_ref[:, 2 * channels :], preferred_element_type=wide)
            + table_ref[15:16, :]
        ).astype(jnp.bfloat16)
        value_ref[rows, :] = values
        value_flip_ref[:, rows] = values.T

    normalise(0)
    for start in range(0, pixels, KEY_ROWS):
        if start + KEY_ROWS < pixels:
            normalise(start + KEY_ROWS)
        project(start)
    block = scores_refs[0].shape[1]
    steps = range(0, pixels, KEY_ROWS)

    def score(index):
        rows = slice(index * block, (index + 1) * block)
        for start in steps:
            keys = slice(start, start + KEY_ROWS)
            scores = lax.dot_general(
                key_ref[keys, :],
                query_ref[rows, :],
                (((1,), (1,)), ((), ())),
                preferred_element_type=wide,
            )
            same = widen(id_rows_ref[keys, :], block) == id_cols_ref[0:1, rows]
            scores_refs[index][keys, :] = jnp.where(same, scores, masked_score)

    def soften(index):
        rows = slice(index * block, (index + 1) * block)
        scores_ref = scores_refs[index]
        peak = jnp.full((8, block), masked_score, wide)
        for start in steps:
            scores = scores_ref[start : start + KEY_ROWS, :]
            peak = jnp.maximum(peak, jnp.max(scores.reshape(-1, 8, block), axis=0))
        peak = jnp.max(peak, axis=0, keepdims=True)
        total = jnp.zeros((8, block), wide)
        for start in steps:
            keys = slice(start, start + KEY_ROWS)
            powers = jnp.exp2((scores_ref[keys, :] - peak) * exponent)
            scores_ref[keys, :] = powers
            total = total + fold(powers)
        share = 1.0 / column_total(total)
        for start in steps:
            keys = slice(start, start + KEY_ROWS)
            soft_ref[keys, rows] = (scores_ref[keys, :] * share).astype(jnp.bfloat16)

    score(0)
    for index in range(len(scores_refs)):
        if index + 1 < len(scores_refs):
            score(index + 1)
        soften(index)

    def collect(rows, carry):
        out_flip_ref[rows, :] = jnp.dot(
            value_flip_ref[rows, :], soft_ref[...], preferred_element_type=wide
        ).astype(jnp.bfloat16)
        return carry

    each_block(channels, channels // 2, collect)
    height = lax.axis_index("height")
    own = pl.ds(pl.multiple_of(height * own_pixels, own_pixels), own_pixels)
    output_ref[...] = (
        residual_ref[own, :]
        + lax.dot_general(
            out_flip_ref[:, own],
            proj_ref[...],
            (((0,), (0,)), ((), ())),
            preferred_element_type=wide,
        )
        + table_ref[16:17, :]
    ).astype(jnp.bfloat16)


def own_quarter():
    height = lax.axis_index("height")
    return (height & 1) * 2 + ((height >> 1) & 1)


def attention_kernel(
    proj_ref,
    normed_ref,
    query_ref,
    key_ref,
    value_ref,
    soft_ref,
    out_flip_ref,
    *refs,
    score_scale,
    count,
):
    pieces, (grad_ref, packed_ref, sums_ref), refs = (
        refs[:count],
        refs[count : count + 3],
        refs[count + 3 :],
    )
    pixels, channels = normed_ref.shape
    blocks = pixels // SCORE_ROWS
    grads_refs, refs = refs[-blocks:], refs[:-blocks]
    keep_ref, send_ref, mixed_ref, key_flip_ref, back_ref, score_grad_ref, flip_ref, sems = refs
    wide = jnp.float32
    copies = place_pieces(pieces, grad_ref, sems)
    for copy in copies:
        copy.start()
    quarter = channels // 4
    own = pl.ds(pl.multiple_of(own_quarter() * quarter, quarter), quarter)
    flip_ref[...] = normed_ref[:, own].T
    key_flip_ref[...] = key_ref[...].T
    for copy in copies:
        copy.wait()
    block, count = SCORE_ROWS, blocks
    steps = range(0, pixels, KEY_ROWS)

    def block_rows(index):
        return slice(index * block, (index + 1) * block)

    for index in range(count):
        back_ref[block_rows(index), :] = lax.dot_general(
            grad_ref[block_rows(index), :],
            proj_ref[...],
            (((1,), (1,)), ((), ())),
            preferred_element_type=wide,
        ).astype(jnp.bfloat16)

    def weigh(index):
        total = jnp.zeros((8, block), wide)
        for start in steps:
            keys = slice(start, start + KEY_ROWS)
            weight_grad = lax.dot_general(
                value_ref[keys, :],
                back_ref[block_rows(index), :],
                (((1,), (1,)), ((), ())),
                preferred_element_type=wide,
            )
            grads_refs[index][keys, :] = weight_grad
            total = total + fold(soft_ref[keys, block_rows(index)].astype(wide) * weight_grad)
        return column_total(total)

    def slope(index, dots):
        for start in steps:
            keys = slice(start, start + KEY_ROWS)
            weights = soft_ref[keys, block_rows(index)].astype(wide)
            score_grad_ref[keys, block_rows(index)] = (
                weights * (grads_refs[index][keys, :] - dots)
            ).astype(jnp.bfloat16)

    dots = weigh(0)
    for index in range(count):
        now, rows = dots, block_rows(index)
        if index + 1 < count:
            dots = weigh(index + 1)
        slope(index, now)
        packed_ref[rows, 2 * channels :] = jnp.dot(
            soft_ref[rows, :], back_ref[...], preferred_element_type=wide
        ).astype(jnp.bfloat16)
        query_grad = jnp.dot(
            key_flip_ref[...], score_grad_ref[:, rows], preferred_element_type=wide
        )
        packed_ref[rows, 0:channels] = (query_grad * score_scale).astype(jnp.bfloat16).T
    for index in range(count):
        rows = block_rows(index)
        packed_ref[rows, channels : 2 * channels] = (
            jnp.dot(score_grad_ref[rows, :], query_ref[...], preferred_element_type=wide)
            * score_scale
        ).astype(jnp.bfloat16)

    def pack(rows, carry):
        return (
            carry[0] + fold(packed_ref[rows, 0:channels].astype(wide)),
            carry[1] + fold(packed_ref[rows, 2 * channels :].astype(wide)),
            carry[2] + fold(grad_ref[rows, :].astype(wide)),
        )

    zeros = jnp.zeros((8, channels), wide)
    totals = zeros, zeros, zeros
    for start in range(0, pixels, CHUNK):
        totals = pack(pl.ds(start, CHUNK), totals)
    sums_ref[...] = jnp.zeros(sums_ref.shape, wide)
    for row, total in enumerate(totals):
        sums_ref[8 + row : 9 + row, :] = column_total(total)
    mixed_ref[:, 0 : 3 * channels] = jnp.dot(
        flip_ref[...], packed_ref[...], preferred_element_type=wide
    ).astype(jnp.bfloat16)
    mixed_ref[:, 3 * channels :] = jnp.dot(
        out_flip_ref[own, :], grad_ref[...], preferred_element_type=wide
    ).astype(jnp.bfloat16)
    keep_half(mixed_ref, 0, keep_ref, send_ref)


def third_kernel(
    qkv_ref,
    grad_ref,
    packed_ref,
    residual_ref,
    table_ref,
    act_two_ref,
    lanes_ref,
    old_sums_ref,
    residual_grad_ref,
    grad_two_ref,
    sums_ref,
    part_ref,
    total_ref,
    flip_ref,
    columns_ref,
    *,
    cols,
):
    pixels, channels = residual_ref.shape
    block = FILL_ROWS
    wide = jnp.float32
    mean, inverse, gain, shift = norm_rows(table_ref, 2)
    zeros = jnp.zeros((8, channels), wide)

    sums = (zeros, zeros)
    for start in range(0, pixels, block):
        rows = pl.ds(start, block)
        normed_grad = lax.dot_general(
            packed_ref[rows, :], qkv_ref[...], (((1,), (1,)), ((), ())), preferred_element_type=wide
        )
        total_ref[rows, :] = normed_grad
        centered = residual_ref[rows, :] - mean
        sums = sums[0] + fold(normed_grad), sums[1] + fold(normed_grad * centered)
    sums = sums[0], sums[1] * inverse
    sums_ref[...] = old_sums_ref[...]
    sums_ref[5:6, :] = column_total(sums[1])
    sums_ref[6:7, :] = column_total(sums[0])
    back = norm_back(
        total_ref, False, sums, lambda rows: residual_ref[rows, :], table_ref, 2, pixels
    )

    def finish(rows, carry):
        total = grad_ref[rows, :].astype(wide) + back(rows, rows)
        residual_grad_ref[rows, :] = total
        low = total.astype(jnp.bfloat16)
        grad_two_ref[rows, :] = low
        return carry + fold(low.astype(wide))

    sums_ref[7:8, :] = column_total(each_chunk(pixels, finish, zeros))
    narrow = grad_two_ref[:, own_lanes()]
    weight_part(act_two_ref, narrow, lanes_ref, flip_ref, columns_ref, part_ref, cols)


def second_kernel(
    old_total_ref,
    taps_ref,
    middle_ref,
    table_ref,
    act_one_ref,
    mask_ref,
    lanes_ref,
    weights_ref,
    old_sums_ref,
    part_two_ref,
    grad_one_ref,
    sums_ref,
    keep_one_ref,
    send_one_ref,
    keep_two_ref,
    send_two_ref,
    total_ref,
    flip_ref,
    columns_ref,
    part_ref,
    scales_ref,
    *,
    cols,
):
    pixels, channels = middle_ref.shape

    def read(rows):
        return middle_ref[rows, :]

    sums = finish_back(
        weights_ref.at[1], mask_ref, taps_ref, total_ref, read, table_ref, 1, cols, old_total_ref
    )
    back = norm_back(total_ref, True, sums, read, table_ref, 1, pixels, scales_ref)
    narrow = narrow_back(total_ref, middle_ref, scales_ref).astype(jnp.bfloat16)
    weight_part(act_one_ref, narrow, lanes_ref, flip_ref, columns_ref, part_ref, cols)
    sums_ref[...] = old_sums_ref[...]
    sums_ref[2:3, :] = column_total(sums[1])
    sums_ref[3:4, :] = column_total(sums[0])

    def finish(rows, carry):
        low = back(rows, rows).astype(jnp.bfloat16)
        grad_one_ref[rows, :] = low
        return carry + fold(low.astype(jnp.float32))

    zeros = jnp.zeros((8, channels), jnp.float32)
    sums_ref[4:5, :] = column_total(each_chunk(pixels, finish, zeros))
    keep_half(part_ref, 1, keep_one_ref, send_one_ref)
    keep_half(part_two_ref, 1, keep_two_ref, send_two_ref)


def near_far():
    core = lax.axis_index("height") & 1
    return 1 + core, 2 - core


def keep_half(source_ref, axis, keep_ref, send_ref):
    me = lax.axis_index("canvas")
    near, far = near_far()
    rows, width = keep_ref.shape[0] // 2, keep_ref.shape[1]
    for target_ref, flip in ((keep_ref, 0), (send_ref, near)):
        for slot, other in enumerate((0, far)):
            owner = me ^ flip ^ other
            target = target_ref.at[slot * rows : (slot + 1) * rows, :]
            if axis == 0:
                target[...] = source_ref[pl.ds(pl.multiple_of(owner * rows, rows), rows), :]
            else:
                target[...] = source_ref[:, pl.ds(pl.multiple_of(owner * width, width), width)]


def first_kernel(
    grad_one_ref,
    features_ref,
    table_ref,
    mask_ref,
    old_sums_ref,
    weights_ref,
    own_ref,
    sums_ref,
    partial_ref,
    total_ref,
    taps_ref,
    *,
    cols,
):
    def read(rows):
        return features_ref[rows, :].astype(jnp.float32)

    weights = weights_ref.at[0]
    begin_back(grad_one_ref, weights, mask_ref, taps_ref, total_ref, cols)
    sums = finish_back(weights, mask_ref, taps_ref, total_ref, read, table_ref, 0, cols)
    partial_ref[0:8, :], partial_ref[8:16, :] = sums
    sums_ref[...] = old_sums_ref[...]
    sums_ref[0:1, :] = column_total(sums[1])
    sums_ref[1:2, :] = column_total(sums[0])
    count = own_ref.shape[0]
    own = pl.ds(pl.multiple_of(lax.axis_index("height") * count, count), count)
    own_ref[...] = total_ref[own, :]


def own_kernel(
    own_ref, partial_ref, features_ref, residual_grad_ref, table_ref, input_grad_ref
):
    def read(rows):
        return features_ref[rows, :].astype(jnp.float32)

    sums = partial_ref[0:8, :], partial_ref[8:16, :]
    pixels = features_ref.shape[0]
    back = norm_back(own_ref, True, sums, read, table_ref, 0, pixels)
    count = own_ref.shape[0]
    own = pl.ds(pl.multiple_of(lax.axis_index("height") * count, count), count)
    total = residual_grad_ref[own, :] + back(own, slice(0, count))
    input_grad_ref[...] = total.astype(jnp.bfloat16)


def place_kernel(*refs):
    joints, packed_ref = refs[:-1], refs[-1]
    share = packed_ref.shape[0] // len(joints)
    me = lax.axis_index("canvas")
    for step, joint in enumerate(joints):
        place = pl.ds(pl.multiple_of((me ^ step) * share, share), share)
        packed_ref[place, :] = joint[...]


def cut_kernel(packed_ref, *half_refs):
    rows = half_refs[0].shape[0]
    for index, half_ref in enumerate(half_refs):
        half_ref[...] = packed_ref[index * rows : (index + 1) * rows, :]


def spread_quarters(packed, flips, qkv_ref, proj_ref, qkv_hbm, proj_hbm, sems):
    quarter = packed[0].shape[0]
    inner = qkv_ref.shape[2]
    copies = []
    for index, packed_ref in enumerate(packed):
        owner = own_quarter() ^ flips[index]
        rows = pl.ds(pl.multiple_of(owner * quarter, quarter), quarter)
        qkv_ref[index] = packed_ref[:, 0:inner].astype(jnp.float32)
        proj_ref[index] = packed_ref[:, inner:].astype(jnp.float32)
        for which, (held, target) in enumerate(((qkv_ref, qkv_hbm), (proj_ref, proj_hbm))):
            copy = pltpu.make_async_copy(held.at[index], target.at[rows, :], sems.at[index, which])
            copy.start()
            copies.append(copy)
    return copies


def join_kernel(*refs):
    packed, (qkv_hbm, proj_hbm, qkv_ref, proj_ref, sems) = refs[:-5], refs[-5:]
    copies = spread_quarters(packed, [0, 2], qkv_ref, proj_ref, qkv_hbm, proj_hbm, sems)
    for copy in copies:
        copy.wait()


def halve_kernel(keep_ref, got_ref, hold_ref, send_ref):
    total = keep_ref[...].astype(jnp.float32) + got_ref[...].astype(jnp.float32)
    rows = hold_ref.shape[0]
    hold_ref[...] = total[0:rows]
    send_ref[0:rows, :] = total[rows:].astype(jnp.bfloat16)


def halve_both_kernel(
    keep_ref, got_ref, keep_two_ref, got_two_ref, hold_ref, send_ref, hold_two_ref
):
    rows = hold_ref.shape[0]
    halve_kernel(keep_ref, got_ref, hold_ref, send_ref)
    halve_kernel(keep_two_ref, got_two_ref, hold_two_ref, send_ref.at[rows : 2 * rows, :])


def last_kernel(
    chip_ref,
    both_a_ref,
    both_b_ref,
    old_qkv,
    old_proj,
    qkv_hbm,
    proj_hbm,
    qkv_ref,
    proj_ref,
    sems,
):
    copies = []
    rows = both_a_ref.shape[0]
    inner = qkv_ref.shape[2]
    chips = (chip_ref.at[0:rows, :], chip_ref.at[rows : 2 * rows, :])
    for index, piece_ref in enumerate((*chips, both_a_ref, both_b_ref)):
        start = ((own_quarter() ^ (1 if index < 2 else 3)) * 2 + index % 2) * rows
        target = pl.ds(pl.multiple_of(start, rows), rows)
        qkv_ref[index] = piece_ref[:, 0:inner].astype(jnp.float32)
        proj_ref[index] = piece_ref[:, inner:].astype(jnp.float32)
        for which, (held, whole) in enumerate(((qkv_ref, qkv_hbm), (proj_ref, proj_hbm))):
            copy = pltpu.make_async_copy(held.at[index], whole.at[target, :], sems.at[index, which])
            copy.start()
            copies.append(copy)
    for copy in copies:
        copy.wait()


def sums_kernel(
    sums_ref,
    got_sums_ref,
    hold_one_ref,
    hold_two_ref,
    got_ref,
    share_ref,
    gains_ref,
    shifts_ref,
    conv_ref,
    qv_ref,
    bias_ref,
):
    rows = hold_one_ref.shape[0]
    for which, hold_ref in enumerate((hold_one_ref, hold_two_ref)):
        got = got_ref[which * rows : (which + 1) * rows, :].astype(jnp.float32)
        share_ref[which] = (hold_ref[...] + got).reshape(share_ref.shape[1:])
    total = sums_ref[...] + got_sums_ref[...]
    for row, start in enumerate((0, 2, 5)):
        gains_ref[row : row + 1, :] = total[start : start + 1]
        shifts_ref[row : row + 1, :] = total[start + 1 : start + 2]
    conv_ref[0:1, :] = total[4:5]
    conv_ref[1:2, :] = total[7:8]
    qv_ref[...] = total[8:10]
    bias_ref[...] = total[10:11]


def call_kernel(kernel, outputs, scratch, operands, places, flops, limit, out_places=None, aliases={}):
    out_places = out_places or "v" * len(outputs)
    spaces = {
        "v": pl.BlockSpec(memory_space=pltpu.VMEM),
        "s": pl.BlockSpec(memory_space=pltpu.SMEM),
        "h": pl.BlockSpec(memory_space=pl.ANY),
        "o": pl.BlockSpec(memory_space=pltpu.VMEM),
        "a": pl.BlockSpec(memory_space=pl.ANY),
    }
    moved = 8 * flops // LANES
    held = {"v": pltpu.VMEM, "h": pltpu.HBM, "o": jax.ShapeDtypeStruct}
    operands = [
        pltpu.with_memory_space_constraint(array, pltpu.HBM) if place == "h" else array
        for array, place in zip(operands, places)
    ]
    return pl.pallas_call(
        kernel,
        out_shape=[held[place](*output) for output, place in zip(outputs, out_places)],
        in_specs=[spaces[place] for place in places],
        out_specs=[spaces[place] for place in out_places],
        scratch_shapes=scratch,
        input_output_aliases=aliases,
        compiler_params=pltpu.CompilerParams(vmem_limit_bytes=limit * 2**20),
        cost_estimate=pl.CostEstimate(flops=flops, bytes_accessed=moved, transcendentals=0),
    )(*operands)


def send_height(block, step):
    size = lax.axis_size("height")
    return lax.ppermute(block, "height", [(i, i ^ step) for i in range(size)])


def with_cores(blocks, other):
    pieces = [blocks[0], other]
    for block in blocks[1:]:
        pieces += [block, send_height(block, 1)]
    return pieces


def send_canvas(block, step):
    size = lax.axis_size("canvas")
    return lax.ppermute(block, "canvas", [(i, i ^ step) for i in range(size)])


def send_phase(block, phase):
    canvases, size = lax.axis_size("canvas"), lax.axis_size("height")
    pairs = []
    for canvas in range(canvases):
        for height in range(size):
            step = 2 if (height ^ phase) & 1 else 1
            pairs.append((canvas * size + height, (canvas ^ step) * size + height))
    return lax.ppermute(block, ("canvas", "height"), pairs)


def trade_canvas(pieces):
    return [pieces[0]] + [send_canvas(piece, step) for step, piece in enumerate(pieces) if step]


def whole_canvas(
    features,
    tile_ids,
    norm_gains,
    norm_shifts,
    conv_weights,
    conv_biases,
    qkv_weight,
    qv_bias,
    proj_weight,
    proj_bias,
    cotangent,
):
    height_size = lax.axis_size("height")
    canvas_size = lax.axis_size("canvas")
    local_rows, cols, channels = features.shape[1:]
    all_rows = tile_ids.shape[1]
    pixels = all_rows * cols
    own_pixels = local_rows * cols
    out_share = channels // height_size
    ci_share = channels // canvas_size
    quarter = channels // 4
    row_share = quarter // canvas_size
    low, wide = jnp.bfloat16, jnp.float32

    own_features = features.reshape(own_pixels, channels)
    own_grad = cotangent.reshape(own_pixels, channels)
    steps = range(2, height_size, 2)
    held_features = [own_features] + [send_height(own_features, step) for step in steps]
    plane = ((pixels, channels), low)
    plane_wide = ((pixels, channels), wide)
    sums_shape = ((16, channels), wide)
    mixed_halves = [((2 * row_share, 4 * channels), low)] * 2
    taps = pltpu.VMEM((pixels + 2 * cols, 3 * channels), low)
    held_wide = pltpu.VMEM((pixels, channels), wide)
    flipped = pltpu.VMEM((channels, pixels), low)
    narrow = pltpu.VMEM((NARROW, pixels), low)
    columns = pltpu.VMEM((9 * out_share, pixels), low)
    part_held = pltpu.VMEM((9 * out_share, channels), low)
    sem = pltpu.SemaphoreType.DMA
    conv_flops = 2 * 9 * pixels * channels * channels
    dot_flops = 2 * pixels * channels * channels
    score_flops = 2 * pixels * pixels * channels
    scale = channels ** (-0.5)

    (
        held_conv,
        turned,
        held_qkv,
        held_proj,
        params,
        mask,
        lane_mask,
        id_rows,
        id_cols,
    ) = call_kernel(
        functools.partial(hold_kernel, cols=cols),
        [
            (conv_weights.shape, low),
            ((2, 3, channels, 3 * channels), low),
            (qkv_weight.shape, low),
            (proj_weight.shape, low),
            ((24, channels), wide),
            ((2, pixels, LANES), wide),
            ((8, pixels), wide),
            ((pixels, LANES), jnp.int32),
            ((8, pixels), jnp.int32),
        ],
        [
            pltpu.SMEM(tile_ids.shape, jnp.int32),
            pltpu.VMEM(norm_gains.shape, wide),
            pltpu.VMEM(norm_shifts.shape, wide),
            pltpu.VMEM(conv_biases.shape, wide),
            pltpu.VMEM(qv_bias.shape, wide),
            pltpu.VMEM((1, channels), wide),
            sem((27,)),
        ],
        [
            tile_ids,
            norm_gains,
            norm_shifts,
            conv_biases,
            conv_weights,
            qkv_weight,
            proj_weight,
            qv_bias,
            proj_bias.reshape(1, channels),
        ],
        "h" * 9,
        conv_flops,
        8,
    )
    held_features[1:] = [
        lax.optimization_barrier((params, block))[1] for block in held_features[1:]
    ]
    other_core = send_height(jnp.concatenate([own_features, own_grad], axis=0), 1)
    pieces = with_cores(held_features, other_core)
    far_grad, *pieces[4::2] = lax.optimization_barrier((own_grad, *held_features[2:]))
    held_grads = [own_grad, send_height(own_grad, 2)]
    held_grads[1], pieces[2] = lax.optimization_barrier((held_grads[1], held_features[1]))
    held_grads += [send_height(far_grad, step) for step in steps[1:]]

    all_features, act_one, middle, act_two, residual, table = call_kernel(
        functools.partial(conv_kernel, cols=cols, count=height_size),
        [plane, plane, plane_wide, plane, plane_wide, ((24, channels), wide)],
        [pltpu.VMEM((own_pixels, channels), low), taps, sem],
        [*pieces, held_conv, params, mask],
        "h" + "v" * (height_size + 2),
        2 * conv_flops,
        16,
    )
    residual, *held_grads = lax.optimization_barrier((residual, *held_grads))
    grad_pieces = with_cores(held_grads, other_core)
    normed, query, key, value, soft, out_flip, output = call_kernel(
        functools.partial(score_kernel, score_scale=scale),
        [
            plane,
            plane,
            plane,
            plane,
            ((pixels, pixels), low),
            ((channels, pixels), low),
            ((own_pixels, channels), low),
        ],
        [
            flipped,
            *[pltpu.VMEM((pixels, SCORE_ROWS), wide)] * (pixels // SCORE_ROWS),
        ],
        [
            held_qkv,
            held_proj,
            residual,
            table,
            id_rows,
            id_cols,
        ],
        "vvvvvv",
        3 * dot_flops + 2 * score_flops,
        20,
        "v" * 6 + "o",
    )
    normed, *grad_pieces = lax.optimization_barrier((normed, *grad_pieces))
    all_grad, packed, sums, keep_mixed, send_mixed = call_kernel(
        functools.partial(attention_kernel, score_scale=scale, count=height_size),
        [plane, ((pixels, 3 * channels), low), sums_shape, *mixed_halves],
        [
            pltpu.VMEM((quarter, 4 * channels), low),
            flipped,
            pltpu.VMEM((pixels, channels), low),
            pltpu.VMEM((pixels, pixels), low),
            pltpu.VMEM((quarter, pixels), low),
            sem((height_size,)),
            *[pltpu.VMEM((pixels, SCORE_ROWS), wide)] * (pixels // SCORE_ROWS),
        ],
        [held_proj, normed, query, key, value, soft, out_flip, *grad_pieces],
        "vvvvvvvh" + "a" * (height_size - 1),
        3 * dot_flops + 4 * score_flops,
        20,
    )
    got_mixed = send_phase(send_mixed, 0)
    residual_grad, grad_two, sums, part_two = call_kernel(
        functools.partial(third_kernel, cols=cols),
        [plane_wide, plane, sums_shape, ((9 * out_share, channels), low)],
        [held_wide, narrow, columns],
        [held_qkv, all_grad, packed, residual, table, act_two, lane_mask, sums],
        "vvvvvvvv",
        3 * dot_flops + conv_flops // height_size,
        16,
    )
    grad_two, got_mixed = lax.optimization_barrier((grad_two, got_mixed))
    hold_mixed, send_mixed = call_kernel(
        halve_kernel,
        [((row_share, 4 * channels), kind) for kind in (wide, low)],
        [],
        [keep_mixed, got_mixed],
        "vv",
        1,
        12,
    )
    got_mixed = send_phase(send_mixed, 1)
    grad_two, hold_mixed = lax.optimization_barrier((grad_two, hold_mixed))
    half_total, half_taps = call_kernel(
        functools.partial(turn_kernel, cols=cols),
        [plane_wide, (taps.shape, low)],
        [],
        [grad_two, mask, turned],
        "vvv",
        2 * conv_flops // 3,
        16,
    )
    half_total, got_mixed = lax.optimization_barrier((half_total, got_mixed))
    mixed_sum = (hold_mixed + got_mixed.astype(wide)).astype(low)
    joints = trade_canvas([mixed_sum] * canvas_size)
    halves = [((2 * 9 * out_share, ci_share), low)] * 4
    grad_one, sums, keep_one, send_one, keep_two, send_two = call_kernel(
        functools.partial(second_kernel, cols=cols),
        [plane, sums_shape, *halves],
        [held_wide, narrow, columns, part_held, pltpu.VMEM((8, channels), wide)],
        [half_total, half_taps, middle, table, act_one, mask, lane_mask, turned, sums, part_two],
        "v" * 10,
        conv_flops // 2,
        20,
    )
    grad_one, *joints = lax.optimization_barrier((grad_one, *joints))
    (own_mixed,) = call_kernel(
        place_kernel,
        [((quarter, 4 * channels), low)],
        [],
        joints,
        "v" * canvas_size,
        1,
        12,
    )
    own_mixed, send_one, send_two = lax.optimization_barrier((own_mixed, send_one, send_two))
    chip_mixed = send_height(own_mixed, 2)
    core_mixed = send_height(own_mixed, 1)
    got_one, got_two = send_phase(send_one, 0), send_phase(send_two, 0)
    own_total, sums, partial_sums = call_kernel(
        functools.partial(first_kernel, cols=cols),
        [((own_pixels, channels), wide), sums_shape, sums_shape],
        [held_wide, taps],
        [grad_one, all_features, table, mask, sums, turned],
        "vvvvvv",
        1,
        20,
    )
    got_sums = send_phase(sums, 0)
    (input_grad,) = call_kernel(
        own_kernel,
        [((own_pixels, channels), low)],
        [],
        [own_total, partial_sums, all_features, residual_grad, table],
        "vvvvv",
        dot_flops // 4,
        12,
        "o",
    )
    input_grad, core_mixed, got_one, got_two = lax.optimization_barrier(
        (input_grad, core_mixed, got_one, got_two)
    )
    share_rows = 9 * out_share
    hold_one, send_share, hold_two = call_kernel(
        halve_both_kernel,
        [
            ((share_rows, ci_share), wide),
            ((2 * share_rows, ci_share), low),
            ((share_rows, ci_share), wide),
        ],
        [],
        [keep_one, got_one, keep_two, got_two],
        "vvvv",
        1,
        12,
    )
    got_share = send_phase(send_share, 1)
    got_sums, hold_one = lax.optimization_barrier((got_sums, hold_one))
    sums = sums + got_sums
    got_sums = send_phase(sums, 1)

    def widened(count, rows):
        return [
            pltpu.VMEM((count, rows, 3 * channels), wide),
            pltpu.VMEM((count, rows, channels), wide),
            sem((count, 2)),
        ]

    grad_shapes = [(qkv_weight.shape, wide), (proj_weight.shape, wide)]
    core_mixed, hold_one = lax.optimization_barrier((core_mixed, hold_one))
    qkv_grad, proj_grad = call_kernel(
        join_kernel,
        grad_shapes,
        widened(2, quarter),
        [own_mixed, core_mixed],
        "vv",
        1,
        12,
        "hh",
    )
    qkv_grad, chip_mixed = lax.optimization_barrier((qkv_grad, chip_mixed))
    chip_halves = call_kernel(
        cut_kernel,
        [((quarter // 2, 4 * channels), low)] * 2,
        [],
        [chip_mixed],
        "v",
        1,
        12,
    )
    both_halves = [send_height(half, 1) for half in chip_halves]
    qkv_grad, proj_grad = call_kernel(
        last_kernel,
        grad_shapes,
        widened(4, quarter // 2),
        [chip_mixed, *both_halves, qkv_grad, proj_grad],
        "vvvhh",
        1,
        12,
        "hh",
        {3: 0, 4: 1},
    )
    qkv_grad, got_share, got_sums = lax.optimization_barrier((qkv_grad, got_share, got_sums))
    vector_shapes = [norm_gains.shape, norm_shifts.shape, conv_biases.shape, qv_bias.shape]
    conv_grad, gains_grad, shifts_grad, biases_grad, qv_grad, proj_bias_grad = call_kernel(
        sums_kernel,
        [((2, 3, 3, out_share, ci_share), wide)]
        + [(shape, wide) for shape in vector_shapes + [(1, channels)]],
        [],
        [sums, got_sums, hold_one, hold_two, got_share],
        "vvvvv",
        1,
        12,
        "o" * 6,
    )
    own_shape = (1, local_rows, cols, channels)
    return (
        output.reshape(own_shape),
        input_grad.reshape(own_shape),
        gains_grad,
        shifts_grad,
        jnp.swapaxes(conv_grad, 3, 4),
        biases_grad,
        qkv_grad,
        qv_grad,
        proj_grad,
        proj_bias_grad.reshape(channels),
    )


def on_device(*arrays):
    features, tile_ids = arrays[0], arrays[1]
    local_rows, cols, channels = features.shape[1:]
    pixels = tile_ids.shape[1] * cols
    height_size, canvas_size = lax.axis_size("height"), lax.axis_size("canvas")
    powers = all(size & (size - 1) == 0 for size in (height_size, canvas_size, cols))
    fits = (
        powers
        and height_size > 2
        and canvas_size == 4
        and channels == LANES * canvas_size
        and pixels <= MOST_PIXELS
        and pixels % FILL_ROWS == 0
        and FILL_ROWS % CHUNK == 0
        and pixels % SCORE_ROWS == 0
        and pixels % KEY_ROWS == 0
        and (local_rows * cols) % LANES == 0
        and CHUNK % cols == 0
        and cols % 16 == 0
        and channels % (LANES * canvas_size) == 0
        and 2 * channels == NARROW * height_size
    )
    return whole_canvas(*arrays) if fits else split_canvas(*arrays)


def solution(mesh):
    in_specs = (
        P("canvas", "height", None, None),
        P("canvas", None),
        P(),
        P(),
        P(),
        P(),
        P(),
        P(),
        P(),
        P(),
        P("canvas", "height", None, None),
    )
    out_specs = (
        P("canvas", "height", None, None),
        P("canvas", "height", None, None),
        P(),
        P(),
        P(None, None, None, "canvas", "height"),
        P(),
        P(),
        P(),
        P(),
        P(),
    )
    return jax.shard_map(
        on_device, mesh=mesh, in_specs=in_specs, out_specs=out_specs, check_vma=False
    )
```

```python
import functools

import jax
import jax.numpy as jnp
from jax import lax
from jax.experimental import pallas as pl
from jax.experimental.pallas import tpu as pltpu
from jax.sharding import PartitionSpec as P

GROUPS = 32


epsilon = 1e-06
masked_score = -1e30
MOST_PIXELS = 1024
LANES = 128
NARROW = 128
CHUNK = 128
FILL_ROWS = 256
QUERY_ROWS = 512
SCORE_ROWS = 256
KEY_ROWS = 512


def extended(block, sides, width):
    for axis, dim in sides:
        count = lax.axis_size(axis)
        forward = [(i, i + 1) for i in range(count - 1)]
        backward = [(target, source) for source, target in forward]
        low = lax.ppermute(
            lax.slice_in_dim(block, block.shape[dim] - width, None, axis=dim), axis, forward
        )
        high = lax.ppermute(lax.slice_in_dim(block, 0, width, axis=dim), axis, backward)
        block = jnp.concatenate([low, block, high], axis=dim)
    return block


def group_total(vector):
    return vector.reshape(GROUPS, -1).sum(axis=1)


def spread_groups(vector, channels):
    return jnp.repeat(vector, channels // GROUPS)


def norm_forward(values, gain, shift, members):
    channels = values.shape[1]
    totals = lax.psum(group_total(jnp.sum(values, axis=0)), "height")
    centered = values - spread_groups(totals / members, channels)
    squares = lax.psum(group_total(jnp.sum(centered * centered, axis=0)), "height")
    inverse = spread_groups(lax.rsqrt(squares / members + epsilon), channels)
    normed = centered * inverse
    return (normed, inverse, normed * gain + shift)


def norm_backward(grad_in, normed, inverse, gain, members):
    channels = grad_in.shape[1]
    scaled = grad_in * gain
    both_sums = lax.psum(
        (group_total(jnp.sum(scaled, axis=0)), group_total(jnp.sum(scaled * normed, axis=0))),
        "height",
    )
    mean_grad = spread_groups(both_sums[0] / members, channels)
    mean_cross = spread_groups(both_sums[1] / members, channels)
    result = inverse * (scaled - mean_grad - normed * mean_cross)
    return (result, jnp.sum(grad_in * normed, axis=0), jnp.sum(grad_in, axis=0))


def swish(values):
    return values * jax.nn.sigmoid(values)


def swish_slope(values):
    sigmoid_part = jax.nn.sigmoid(values)
    return sigmoid_part * (1.0 + values * (1.0 - sigmoid_part))


def tap_columns(padded, row_mask, local_rows, canvas_cols):
    pieces = []
    for row_tap in range(3):
        rows_taken = padded[row_tap : row_tap + local_rows] * row_mask[:, row_tap, None, None]
        for col_tap in range(3):
            pieces.append(rows_taken[:, col_tap : col_tap + canvas_cols])
    stacked = jnp.concatenate(pieces, axis=2)
    return stacked.reshape(local_rows * canvas_cols, stacked.shape[2])


def conv_forward(acts, row_mask, weight, bias):
    local_rows, canvas_cols, channels = acts.shape
    rimmed = extended(acts, (("height", 0),), 1)
    padded = jnp.pad(rimmed, ((0, 0), (1, 1), (0, 0)))
    gathered = tap_columns(padded, row_mask, local_rows, canvas_cols)
    result = (
        jnp.dot(
            gathered, weight.reshape(9 * channels, channels), preferred_element_type=jnp.float32
        )
        + bias
    )
    return (result, gathered)


def conv_backward(grad_low, row_mask, weight, gathered):
    local_rows, canvas_cols, channels = grad_low.shape
    flat_grad = grad_low.reshape(local_rows * canvas_cols, channels)
    weight_grad = lax.dot_general(
        gathered, flat_grad, (((0,), (0,)), ((), ())), preferred_element_type=jnp.float32
    )
    rimmed = extended(grad_low, (("height", 0),), 1)
    padded = jnp.pad(rimmed, ((0, 0), (1, 1), (0, 0)))
    grad_taps = tap_columns(padded, row_mask, local_rows, canvas_cols)
    flipped = jnp.transpose(weight[::-1, ::-1], (0, 1, 3, 2)).reshape(9 * channels, channels)
    input_part = jnp.dot(grad_taps, flipped, preferred_element_type=jnp.float32)
    return (
        input_part,
        weight_grad.reshape(3, 3, channels, channels),
        jnp.sum(flat_grad.astype(jnp.float32), axis=0),
    )


def take_rows(array, offset, count):
    return lax.dynamic_slice_in_dim(array, offset, count)


def score_grads(
    queries, out_grad, log_total, row_dots, query_ids, key_rows, value_rows, key_ids, score_scale
):
    scores = (
        lax.dot_general(
            queries, key_rows, (((1,), (1,)), ((), ())), preferred_element_type=jnp.float32
        )
        * score_scale
    )
    same_tile = query_ids[:, None] == key_ids[None, :]
    softmax_block = jnp.exp(jnp.where(same_tile, scores - log_total[:, None], masked_score))
    weight_grad = lax.dot_general(
        out_grad, value_rows, (((1,), (1,)), ((), ())), preferred_element_type=jnp.float32
    )
    score_grad = (softmax_block * (weight_grad - row_dots[:, None])).astype(jnp.bfloat16)
    return (softmax_block.astype(jnp.bfloat16), score_grad)


def split_canvas(
    features,
    tile_ids,
    norm_gains,
    norm_shifts,
    conv_weights,
    conv_biases,
    qkv_weight,
    qv_bias,
    proj_weight,
    proj_bias,
    cotangent,
):
    height_size = lax.axis_size("height")
    local_rows = features.shape[1]
    canvas_cols = features.shape[2]
    channels = features.shape[3]
    pixels = local_rows * canvas_cols
    row_ids = tile_ids[0]
    all_rows = row_ids.shape[0]
    members = float(all_rows * canvas_cols * (channels // GROUPS))
    score_scale = channels ** (-0.5)
    first_row = lax.axis_index("height") * local_rows
    edge_ids = jnp.full((1,), -1, jnp.int32)
    padded_ids = jnp.concatenate([edge_ids, row_ids, edge_ids])
    near_ids = lax.dynamic_slice_in_dim(padded_ids, first_row, local_rows + 2)
    own_rows = near_ids[1 : local_rows + 1]
    row_mask = jnp.stack(
        [near_ids[row_tap : row_tap + local_rows] == own_rows for row_tap in range(3)], axis=1
    ).astype(jnp.bfloat16)
    key_ids = jnp.repeat(row_ids, canvas_cols)
    query_ids = jnp.repeat(own_rows, canvas_cols)
    grid_shape = (local_rows, canvas_cols, channels)
    inputs = features[0].reshape(pixels, channels).astype(jnp.float32)
    normed_one, inverse_one, pre_one = norm_forward(inputs, norm_gains[0], norm_shifts[0], members)
    act_one = swish(pre_one).astype(jnp.bfloat16).reshape(grid_shape)
    middle, taps_one = conv_forward(act_one, row_mask, conv_weights[0], conv_biases[0])
    normed_two, inverse_two, pre_two = norm_forward(middle, norm_gains[1], norm_shifts[1], members)
    act_two = swish(pre_two).astype(jnp.bfloat16).reshape(grid_shape)
    branch, taps_two = conv_forward(act_two, row_mask, conv_weights[1], conv_biases[1])
    residual = inputs + branch
    normed_three, inverse_three, pre_three = norm_forward(
        residual, norm_gains[2], norm_shifts[2], members
    )
    attn_input = pre_three.astype(jnp.bfloat16)
    mixed = jnp.dot(attn_input, qkv_weight, preferred_element_type=jnp.float32)
    queries = (mixed[:, :channels] + qv_bias[0]).astype(jnp.bfloat16)
    key_rows = mixed[:, channels : 2 * channels].astype(jnp.bfloat16)
    value_rows = (mixed[:, 2 * channels :] + qv_bias[1]).astype(jnp.bfloat16)
    running_max = jnp.full((pixels,), masked_score, jnp.float32)
    key_piece = lax.all_gather(key_rows, "height", axis=0, tiled=True)
    value_piece = lax.all_gather(value_rows, "height", axis=0, tiled=True)
    scores = (
        lax.dot_general(
            queries, key_piece, (((1,), (1,)), ((), ())), preferred_element_type=jnp.float32
        )
        * score_scale
    )
    same_tile = query_ids[:, None] == key_ids[None, :]
    scores = jnp.where(same_tile, scores, masked_score)
    new_max = jnp.maximum(running_max, jnp.max(scores, axis=1))
    weights = jnp.where(same_tile, jnp.exp(scores - new_max[:, None]), 0.0)
    summed_out = jnp.dot(
        weights.astype(jnp.bfloat16), value_piece, preferred_element_type=jnp.float32
    )
    total_weight = jnp.sum(weights, axis=1)
    log_total = new_max + jnp.log(total_weight)
    attended = summed_out / total_weight[:, None]
    attended_low = attended.astype(jnp.bfloat16)
    output = (
        residual
        + jnp.dot(attended_low, proj_weight, preferred_element_type=jnp.float32)
        + proj_bias
    )
    out_grad = cotangent[0].reshape(pixels, channels)
    out_grad_full = out_grad.astype(jnp.float32)
    proj_grad = lax.dot_general(
        attended_low, out_grad, (((0,), (0,)), ((), ())), preferred_element_type=jnp.float32
    )
    proj_bias_grad = jnp.sum(out_grad_full, axis=0)
    attended_grad = lax.dot_general(
        out_grad, proj_weight, (((1,), (1,)), ((), ())), preferred_element_type=jnp.float32
    ).astype(jnp.bfloat16)
    row_dots = jnp.sum(attended_grad.astype(jnp.float32) * attended, axis=1)
    block_rows = pixels * min(height_size, 8)
    zero_block = jnp.zeros((pixels, channels), jnp.float32)
    key_all, value_all = (
        lax.all_gather(key_rows, "height", axis=0, tiled=True),
        lax.all_gather(value_rows, "height", axis=0, tiled=True),
    )
    query_all, grad_all = (
        lax.all_gather(queries, "height", axis=0, tiled=True),
        lax.all_gather(attended_grad, "height", axis=0, tiled=True),
    )
    total_all, dots_all = (
        lax.all_gather(log_total, "height", axis=0, tiled=True),
        lax.all_gather(row_dots, "height", axis=0, tiled=True),
    )

    def own_query_step(running, block_index):
        offset = block_index * block_rows
        key_part = take_rows(key_all, offset, block_rows)
        rounded, score_grad = score_grads(
            queries,
            attended_grad,
            log_total,
            row_dots,
            query_ids,
            key_part,
            take_rows(value_all, offset, block_rows),
            take_rows(key_ids, offset, block_rows),
            score_scale,
        )
        return (
            running
            + jnp.dot(score_grad, key_part, preferred_element_type=jnp.float32) * score_scale,
            None,
        )

    def own_key_step(running, block_index):
        offset = block_index * block_rows
        query_part = take_rows(query_all, offset, block_rows)
        grad_part = take_rows(grad_all, offset, block_rows)
        rounded, score_grad = score_grads(
            query_part,
            grad_part,
            take_rows(total_all, offset, block_rows),
            take_rows(dots_all, offset, block_rows),
            take_rows(key_ids, offset, block_rows),
            key_rows,
            value_rows,
            query_ids,
            score_scale,
        )
        key_part = (
            lax.dot_general(
                score_grad, query_part, (((0,), (0,)), ((), ())), preferred_element_type=jnp.float32
            )
            * score_scale
        )
        value_part = lax.dot_general(
            rounded, grad_part, (((0,), (0,)), ((), ())), preferred_element_type=jnp.float32
        )
        return ((running[0] + key_part, running[1] + value_part), None)

    block_count = key_all.shape[0] // block_rows
    query_grad, unused_one = lax.scan(own_query_step, zero_block, jnp.arange(block_count))
    (key_grad, value_grad), unused_two = lax.scan(
        own_key_step, (zero_block, zero_block), jnp.arange(block_count)
    )
    query_low = query_grad.astype(jnp.bfloat16)
    key_low = key_grad.astype(jnp.bfloat16)
    value_low = value_grad.astype(jnp.bfloat16)
    stacked_grad = jnp.concatenate([query_low, key_low, value_low], axis=1)
    qkv_grad = lax.dot_general(
        attn_input, stacked_grad, (((0,), (0,)), ((), ())), preferred_element_type=jnp.float32
    )
    qv_grad = jnp.stack(
        [
            jnp.sum(query_low.astype(jnp.float32), axis=0),
            jnp.sum(value_low.astype(jnp.float32), axis=0),
        ]
    )
    normed_grad = lax.dot_general(
        stacked_grad, qkv_weight, (((1,), (1,)), ((), ())), preferred_element_type=jnp.float32
    )
    back_three, gain_three, shift_three = norm_backward(
        normed_grad, normed_three, inverse_three, norm_gains[2], members
    )
    residual_grad = out_grad_full + back_three
    grad_two = residual_grad.astype(jnp.bfloat16).reshape(grid_shape)
    act_two_grad, weight_two_grad, bias_two_grad = conv_backward(
        grad_two, row_mask, conv_weights[1], taps_two
    )
    middle_grad, gain_two, shift_two = norm_backward(
        act_two_grad * swish_slope(pre_two), normed_two, inverse_two, norm_gains[1], members
    )
    grad_one = middle_grad.astype(jnp.bfloat16).reshape(grid_shape)
    act_one_grad, weight_one_grad, bias_one_grad = conv_backward(
        grad_one, row_mask, conv_weights[0], taps_one
    )
    input_back, gain_one, shift_one = norm_backward(
        act_one_grad * swish_slope(pre_one), normed_one, inverse_one, norm_gains[0], members
    )
    input_grad = residual_grad + input_back
    conv_grad = jnp.stack([weight_one_grad, weight_two_grad])
    conv_part = lax.psum_scatter(conv_grad, "height", scatter_dimension=4, tiled=True)
    conv_part = lax.psum_scatter(
        conv_part.astype(jnp.bfloat16), "canvas", scatter_dimension=3, tiled=True
    ).astype(jnp.float32)
    summed = lax.psum(
        (
            jnp.stack([gain_one, gain_two, gain_three]),
            jnp.stack([shift_one, shift_two, shift_three]),
            jnp.stack([bias_one_grad, bias_two_grad]),
            qkv_grad,
            qv_grad,
            proj_grad,
            proj_bias_grad,
        ),
        ("canvas", "height"),
    )
    return (
        output.astype(jnp.bfloat16).reshape((1,) + grid_shape),
        input_grad.astype(jnp.bfloat16).reshape((1,) + grid_shape),
        summed[0],
        summed[1],
        conv_part,
        summed[2],
        summed[3],
        summed[4],
        summed[5],
        summed[6],
    )


def fold(block):
    rows, width = block.shape
    return jnp.sum(block.reshape(rows // 8, 8, width), axis=0)


def group_lanes(block, group):
    lane = lax.broadcasted_iota(jnp.int32, block.shape, 1)
    width = block.shape[1]
    step = 1
    while step < group:
        above = pltpu.roll(block, step, 1)
        below = pltpu.roll(block, width - step, 1)
        block = block + jnp.where((lane & step) != 0, above, below)
        step *= 2
    return block


def group_mean(partial, members):
    spread = group_lanes(partial, partial.shape[1] // GROUPS)
    return jnp.sum(spread, axis=0, keepdims=True) * (1.0 / members)


def widen(block, width):
    return jnp.concatenate([block] * (width // block.shape[1]), axis=1)


def each_block(pixels, block, body, carry=0):
    def step(index, carry):
        return body(pl.ds(pl.multiple_of(index * block, block), block), carry)

    return lax.fori_loop(0, pixels // block, step, carry)


def each_chunk(pixels, body, carry):
    return each_block(pixels, CHUNK, body, carry)


def aligned(start, step):
    return start if isinstance(start, int) else pl.multiple_of(start, step)


class RunningStats:
    def __init__(self, channels):
        self.width = channels // GROUPS
        self.reference = None
        self.sums = self.squares = jnp.zeros((8, channels), jnp.float32)

    def add(self, block):
        if self.reference is None:
            self.reference = group_mean(block[0:8], 8.0 * self.width)
        offset = block - self.reference
        self.sums = self.sums + fold(offset)
        self.squares = self.squares + fold(offset * offset)

    def finish(self, pixels):
        both = group_lanes(jnp.concatenate([self.sums, self.squares], axis=0), self.width)
        share = 1.0 / (pixels * self.width)
        offset = column_total(both[0:8]) * share
        variance = column_total(both[8:16]) * share - offset * offset
        return self.reference + offset, lax.rsqrt(jnp.maximum(variance, 0.0) + epsilon)


def put_taps(taps_ref, block, rows, cols):
    count, channels = block.shape
    place = lax.broadcasted_iota(jnp.int32, block.shape, 0) & (cols - 1)
    left = jnp.where(place == 0, 0.0, pltpu.roll(block, 1, 0))
    right = jnp.where(place == cols - 1, 0.0, pltpu.roll(block, count - 1, 0))
    inner = pl.ds(aligned(rows.start + cols, cols), count)
    taps_ref[inner, 0:channels] = left.astype(jnp.bfloat16)
    taps_ref[inner, channels : 2 * channels] = block.astype(jnp.bfloat16)
    taps_ref[inner, 2 * channels :] = right.astype(jnp.bfloat16)


def clear_edges(taps_ref, cols):
    edge = jnp.zeros((cols, taps_ref.shape[1]), taps_ref.dtype)
    taps_ref[0:cols, :] = edge
    taps_ref[taps_ref.shape[0] - cols :, :] = edge


def begin_conv(taps_ref, product, total_ref, fill, first, cols):
    for start in range(0, total_ref.shape[0], FILL_ROWS):
        for inner in range(start, start + FILL_ROWS, CHUNK):
            fill(pl.ds(inner, CHUNK))
        rows = pl.ds(start, FILL_ROWS)
        total_ref[rows, :] = first(rows, product(taps_ref, pl.ds(start + cols, FILL_ROWS), 1))


def add_rows(taps_ref, product, mask_ref, total_ref, row_tap, last, cols, old_ref=None):
    pixels, channels = total_ref.shape
    old_ref = total_ref if old_ref is None else old_ref

    def step(rows, shifted):
        part = product(taps_ref, shifted, row_tap)
        mask = widen(mask_ref[row_tap // 2, rows, :], channels)
        value = old_ref[rows, :] + mask * part
        total_ref[rows, :] = value if last is None else last(rows, value)

    block = 2 * FILL_ROWS if last is None else FILL_ROWS
    for start in range(0, pixels, block):
        step(pl.ds(start, block), pl.ds(start + row_tap * cols, block))


def run_conv(taps_ref, product, mask_ref, total_ref, fill, first, last, cols):
    begin_conv(taps_ref, product, total_ref, fill, first, cols)
    add_rows(taps_ref, product, mask_ref, total_ref, 0, None, cols)
    add_rows(taps_ref, product, mask_ref, total_ref, 2, last, cols)


def product_forward(weight_ref):
    channels = weight_ref.shape[-1]

    def product(taps_ref, shifted, row_tap):
        return jnp.dot(
            taps_ref[shifted, :],
            weight_ref[row_tap].reshape(3 * channels, channels),
            preferred_element_type=jnp.float32,
        )

    return product


def product_backward(weight_ref):
    def product(taps_ref, shifted, row_tap):
        return lax.dot_general(
            taps_ref[shifted, :],
            weight_ref[row_tap],
            (((1,), (1,)), ((), ())),
            preferred_element_type=jnp.float32,
        )

    return product


def activation(read, mean, inverse, gain, shift, act_ref, taps_ref, cols):
    scale, offset = 0.5 * inverse * gain, 0.5 * shift

    def fill(rows):
        half = (read(rows) - mean) * scale + offset
        act = half * (1.0 + jnp.tanh(half))
        act_ref[rows, :] = act.astype(jnp.bfloat16)
        put_taps(taps_ref, act, rows, cols)

    return fill


def back_means(sums, gain, pixels):
    channels = gain.shape[1]
    members = float(pixels * (channels // GROUPS))
    return group_mean(sums[0] * gain, members), group_mean(sums[1] * gain, members)


def column_total(partial):
    return jnp.sum(partial, axis=0, keepdims=True)


def weight_part(act_ref, narrow, lanes_ref, flip_ref, columns_ref, part_ref, cols):
    pixels, channels = act_ref.shape
    height = lax.axis_index("height")
    share = NARROW // 2
    flip_ref[...] = narrow.T
    own = pl.ds(pl.multiple_of((height % 2) * share, share), share)
    grad = flip_ref[own, :].astype(jnp.float32)
    column = lax.broadcasted_iota(jnp.int32, grad.shape, 1) & (cols - 1)
    for col_tap in range(3):
        shifted = grad
        if col_tap == 0:
            shifted = jnp.where(column == cols - 1, 0.0, pltpu.roll(grad, pixels - 1, 1))
        elif col_tap == 2:
            shifted = jnp.where(column == 0, 0.0, pltpu.roll(grad, 1, 1))
        for row_tap in range(3):
            tap = 3 * row_tap + col_tap
            place = slice(tap * share, (tap + 1) * share)
            if row_tap == 1:
                columns_ref[place, :] = shifted.astype(jnp.bfloat16)
                continue
            side, turn = (0, pixels - cols) if row_tap == 0 else (1, cols)
            masked = (shifted * lanes_ref[side : side + 1, :]).astype(jnp.bfloat16)
            columns_ref[place, :] = pltpu.roll(masked, turn, 1)
    part_ref[...] = jnp.dot(
        columns_ref[...], act_ref[...], preferred_element_type=jnp.float32
    ).astype(jnp.bfloat16)


def begin_back(grad_ref, weights_ref, mask_ref, taps_ref, total_ref, cols):
    clear_edges(taps_ref, cols)

    def fill(rows):
        put_taps(taps_ref, grad_ref[rows, :].astype(jnp.float32), rows, cols)

    product = product_backward(weights_ref)
    begin_conv(taps_ref, product, total_ref, fill, lambda rows, part: part, cols)
    add_rows(taps_ref, product, mask_ref, total_ref, 0, None, cols)


def finish_back(
    weights_ref, mask_ref, taps_ref, total_ref, read, table_ref, which, cols, old_ref=None
):
    mean, inverse, gain, shift = norm_rows(table_ref, which)
    scale, offset = 0.5 * inverse * gain, 0.5 * shift
    sums = []

    def slope(rows, value):
        centered = read(rows) - mean
        half = centered * scale + offset
        turn = jnp.tanh(half)
        double = value * ((1.0 + turn) * (1.0 + half * (1.0 - turn)))
        sums.append((fold(double), fold(double * centered)))
        return double

    add_rows(
        taps_ref, product_backward(weights_ref), mask_ref, total_ref, 2, slope, cols, old_ref
    )
    plain, cross = sum(pair[0] for pair in sums), sum(pair[1] for pair in sums)
    return 0.5 * plain, 0.5 * inverse * cross


def norm_back(total_ref, double, sums, read, table_ref, which, pixels, scales_ref=None):
    mean, inverse, gain, shift = norm_rows(table_ref, which)
    mean_grad, mean_cross = back_means(sums, gain, pixels)
    slope = inverse * gain * (0.5 if double else 1.0)
    level, tilt = inverse * mean_grad, inverse * inverse * mean_cross
    if scales_ref is not None:
        for row, scales in enumerate((mean, slope, level, tilt)):
            scales_ref[row : row + 1, :] = scales

    def back(rows, inner):
        return total_ref[inner, :] * slope - level - (read(rows) - mean) * tilt

    return back


def own_lanes():
    block = lax.axis_index("height") // 2
    return pl.ds(pl.multiple_of(block * NARROW, NARROW), NARROW)


def narrow_back(total_ref, value_ref, scales_ref):
    lanes = own_lanes()
    mean, slope, level, tilt = (scales_ref[row : row + 1, lanes] for row in range(4))
    return total_ref[:, lanes] * slope - level - (value_ref[:, lanes] - mean) * tilt


def turn_kernel(grad_ref, mask_ref, weights_ref, total_ref, taps_ref, *, cols):
    begin_back(grad_ref, weights_ref.at[1], mask_ref, taps_ref, total_ref, cols)


def norm_rows(table_ref, which):
    picks = (2 * which, 2 * which + 1, 6 + which, 9 + which)
    return tuple(table_ref[pick : pick + 1, :] for pick in picks)


def build_masks(ids_ref, mask_ref, lanes_ref, id_rows_ref, id_cols_ref, cols):
    rows = ids_ref.shape[1]

    def one_row(row, carry):
        here = ids_ref[0, row]
        place = pl.ds(pl.multiple_of(row * cols, cols), cols)
        id_rows_ref[place, :] = jnp.full((cols, LANES), here, jnp.int32)
        for side, other in ((0, row - 1), (1, row + 1)):
            inside = jnp.logical_and(other >= 0, other < rows)
            other_id = ids_ref[0, jnp.clip(other, 0, rows - 1)]
            same = jnp.where(jnp.logical_and(inside, other_id == here), 1.0, 0.0)
            mask_ref[side, place, :] = jnp.full((cols, LANES), same, jnp.float32)
        return carry

    lax.fori_loop(0, rows, one_row, 0)
    lane = lax.broadcasted_iota(jnp.int32, (8, LANES), 1)
    each = LANES // cols
    for block in range(rows // each):
        ids = jnp.full((8, LANES), ids_ref[0, block * each], jnp.int32)
        for step in range(1, each):
            ids = jnp.where(lane >= step * cols, ids_ref[0, block * each + step], ids)
        id_cols_ref[:, block * LANES : (block + 1) * LANES] = ids
    ids = id_cols_ref[...].astype(jnp.float32)
    pixels = ids.shape[1]
    pixel = lax.broadcasted_iota(jnp.int32, ids.shape, 1)
    above = jnp.where(pixel < cols, -1.0, pltpu.roll(ids, cols, 1))
    below = jnp.where(pixel >= pixels - cols, -1.0, pltpu.roll(ids, pixels - cols, 1))
    lanes_ref[0:1, :] = jnp.where(above == ids, 1.0, 0.0)[0:1]
    lanes_ref[1:2, :] = jnp.where(below == ids, 1.0, 0.0)[0:1]


def place_pieces(pieces, whole_ref, sems):
    own_pixels = whole_ref.shape[0] // len(pieces)
    height = lax.axis_index("height")
    copies = []
    for place, piece in enumerate(pieces):
        piece = piece.at[piece.shape[0] - own_pixels : piece.shape[0], :]
        start = pl.multiple_of((height ^ place) * own_pixels, own_pixels)
        rows = pl.ds(start, own_pixels)
        copies.append(pltpu.make_async_copy(piece, whole_ref.at[rows, :], sems.at[place]))
    return copies


def hold_kernel(
    ids_hbm,
    gains_hbm,
    shifts_hbm,
    biases_hbm,
    weights_hbm,
    qkv_hbm,
    proj_hbm,
    qv_bias_hbm,
    proj_bias_hbm,
    weights_ref,
    turned_ref,
    qkv_ref,
    proj_ref,
    table_ref,
    mask_ref,
    lanes_ref,
    id_rows_ref,
    id_cols_ref,
    ids_ref,
    gains_ref,
    shifts_ref,
    biases_ref,
    qv_bias_ref,
    proj_bias_ref,
    sems,
    *,
    cols,
):
    channels = weights_ref.shape[-1]
    small = [
        (ids_hbm, ids_ref),
        (gains_hbm, gains_ref),
        (shifts_hbm, shifts_ref),
        (biases_hbm, biases_ref),
        (qv_bias_hbm, qv_bias_ref),
        (proj_bias_hbm, proj_bias_ref),
    ]
    large = [(weights_hbm, weights_ref), (qkv_hbm, qkv_ref), (proj_hbm, proj_ref)]
    for which in range(2):
        for row_tap in range(3):
            for col_tap in range(3):
                place = slice(col_tap * channels, (col_tap + 1) * channels)
                large.append(
                    (
                        weights_hbm.at[which, 2 - row_tap, 2 - col_tap],
                        turned_ref.at[which, row_tap, :, place],
                    )
                )
    copies = [
        pltpu.make_async_copy(source, target, sems.at[index])
        for index, (source, target) in enumerate(small + large)
    ]
    for copy in copies:
        copy.start()
    for copy in copies[: len(small)]:
        copy.wait()
    build_masks(ids_ref, mask_ref, lanes_ref, id_rows_ref, id_cols_ref, cols)
    table_ref[6:9, :] = gains_ref[...]
    table_ref[9:12, :] = shifts_ref[...]
    table_ref[12:14, :] = biases_ref[...]
    table_ref[14:16, :] = qv_bias_ref[...]
    table_ref[16:17, :] = proj_bias_ref[...]
    for copy in copies[len(small) :]:
        copy.wait()


def conv_kernel(*refs, cols, count):
    pieces, refs = refs[:count], refs[count:]
    (
        weights_ref,
        params_ref,
        mask_ref,
        features_ref,
        act_one_ref,
        middle_ref,
        act_two_ref,
        residual_ref,
        table_ref,
        own_ref,
        taps_ref,
        sem,
    ) = refs
    pixels, channels = features_ref.shape
    wide = jnp.float32
    own_copy = pltpu.make_async_copy(pieces[0], own_ref, sem)
    own_copy.start()
    table_ref[...] = params_ref[...]
    clear_edges(taps_ref, cols)

    def read_input(rows):
        return features_ref[rows, :].astype(wide)

    def read_middle(rows):
        return middle_ref[rows, :]

    height = lax.axis_index("height")
    own_pixels = pixels // count
    seen = RunningStats(channels)
    for place in list(range(1, count)) + [0]:
        if place == 0:
            own_copy.wait()
        piece = (pieces[place] if place else own_ref)[0:own_pixels, :]
        start = pl.multiple_of((height ^ place) * own_pixels, own_pixels)
        features_ref[pl.ds(start, own_pixels), :] = piece
        seen.add(piece.astype(wide))
    table_ref[0:1, :], table_ref[1:2, :] = seen.finish(pixels)
    seen = RunningStats(channels)

    def keep(rows, value):
        seen.add(value)
        return value

    run_conv(
        taps_ref,
        product_forward(weights_ref.at[0]),
        mask_ref,
        middle_ref,
        activation(read_input, *norm_rows(table_ref, 0), act_one_ref, taps_ref, cols),
        lambda rows, part: part + table_ref[12:13, :],
        keep,
        cols,
    )
    table_ref[2:3, :], table_ref[3:4, :] = seen.finish(pixels)
    seen = RunningStats(channels)
    run_conv(
        taps_ref,
        product_forward(weights_ref.at[1]),
        mask_ref,
        residual_ref,
        activation(read_middle, *norm_rows(table_ref, 1), act_two_ref, taps_ref, cols),
        lambda rows, part: part + (read_input(rows) + table_ref[13:14, :]),
        keep,
        cols,
    )
    table_ref[4:5, :], table_ref[5:6, :] = seen.finish(pixels)


def score_kernel(
    qkv_ref,
    proj_ref,
    residual_ref,
    table_ref,
    id_rows_ref,
    id_cols_ref,
    normed_ref,
    query_ref,
    key_ref,
    value_ref,
    soft_ref,
    out_flip_ref,
    output_ref,
    value_flip_ref,
    *scores_refs,
    score_scale,
):
    pixels, channels = residual_ref.shape
    own_pixels = output_ref.shape[0]
    wide = jnp.float32
    exponent = score_scale * 1.4426950408889634
    mean, inverse, gain, shift = norm_rows(table_ref, 2)
    scale = inverse * gain

    def normalise(start):
        rows = slice(start, start + KEY_ROWS)
        normed = (residual_ref[rows, :] - mean) * scale + shift
        normed_ref[rows, :] = normed.astype(jnp.bfloat16)

    def project(start):
        rows = slice(start, start + KEY_ROWS)
        normed = normed_ref[rows, :]
        query_ref[rows, :] = (
            jnp.dot(normed, qkv_ref[:, 0:channels], preferred_element_type=wide)
            + table_ref[14:15, :]
        ).astype(jnp.bfloat16)
        key_ref[rows, :] = jnp.dot(
            normed, qkv_ref[:, channels : 2 * channels], preferred_element_type=wide
        ).astype(jnp.bfloat16)
        values = (
            jnp.dot(normed, qkv_ref[:, 2 * channels :], preferred_element_type=wide)
            + table_ref[15:16, :]
        ).astype(jnp.bfloat16)
        value_ref[rows, :] = values
        value_flip_ref[:, rows] = values.T

    normalise(0)
    for start in range(0, pixels, KEY_ROWS):
        if start + KEY_ROWS < pixels:
            normalise(start + KEY_ROWS)
        project(start)
    block = scores_refs[0].shape[1]
    steps = range(0, pixels, KEY_ROWS)

    def score(index):
        rows = slice(index * block, (index + 1) * block)
        for start in steps:
            keys = slice(start, start + KEY_ROWS)
            scores = lax.dot_general(
                key_ref[keys, :],
                query_ref[rows, :],
                (((1,), (1,)), ((), ())),
                preferred_element_type=wide,
            )
            same = widen(id_rows_ref[keys, :], block) == id_cols_ref[0:1, rows]
            scores_refs[index][keys, :] = jnp.where(same, scores, masked_score)

    def soften(index):
        rows = slice(index * block, (index + 1) * block)
        scores_ref = scores_refs[index]
        peak = jnp.full((8, block), masked_score, wide)
        for start in steps:
            scores = scores_ref[start : start + KEY_ROWS, :]
            peak = jnp.maximum(peak, jnp.max(scores.reshape(-1, 8, block), axis=0))
        peak = jnp.max(peak, axis=0, keepdims=True)
        total = jnp.zeros((8, block), wide)
        for start in steps:
            keys = slice(start, start + KEY_ROWS)
            powers = jnp.exp2((scores_ref[keys, :] - peak) * exponent)
            scores_ref[keys, :] = powers
            total = total + fold(powers)
        share = 1.0 / column_total(total)
        for start in steps:
            keys = slice(start, start + KEY_ROWS)
            soft_ref[keys, rows] = (scores_ref[keys, :] * share).astype(jnp.bfloat16)

    score(0)
    for index in range(len(scores_refs)):
        if index + 1 < len(scores_refs):
            score(index + 1)
        soften(index)

    def collect(rows, carry):
        out_flip_ref[rows, :] = jnp.dot(
            value_flip_ref[rows, :], soft_ref[...], preferred_element_type=wide
        ).astype(jnp.bfloat16)
        return carry

    each_block(channels, channels // 2, collect)
    height = lax.axis_index("height")
    own = pl.ds(pl.multiple_of(height * own_pixels, own_pixels), own_pixels)
    output_ref[...] = (
        residual_ref[own, :]
        + lax.dot_general(
            out_flip_ref[:, own],
            proj_ref[...],
            (((0,), (0,)), ((), ())),
            preferred_element_type=wide,
        )
        + table_ref[16:17, :]
    ).astype(jnp.bfloat16)


def own_quarter():
    height = lax.axis_index("height")
    return (height & 1) * 2 + ((height >> 1) & 1)


def attention_kernel(
    proj_ref,
    normed_ref,
    query_ref,
    key_ref,
    value_ref,
    soft_ref,
    out_flip_ref,
    *refs,
    score_scale,
    count,
):
    pieces, (grad_ref, packed_ref, sums_ref), refs = (
        refs[:count],
        refs[count : count + 3],
        refs[count + 3 :],
    )
    pixels, channels = normed_ref.shape
    blocks = pixels // SCORE_ROWS
    grads_refs, refs = refs[-blocks:], refs[:-blocks]
    keep_ref, send_ref, mixed_ref, key_flip_ref, back_ref, score_grad_ref, flip_ref, sems = refs
    wide = jnp.float32
    copies = place_pieces(pieces, grad_ref, sems)
    for copy in copies:
        copy.start()
    quarter = channels // 4
    own = pl.ds(pl.multiple_of(own_quarter() * quarter, quarter), quarter)
    flip_ref[...] = normed_ref[:, own].T
    key_flip_ref[...] = key_ref[...].T
    for copy in copies:
        copy.wait()
    block, count = SCORE_ROWS, blocks
    steps = range(0, pixels, KEY_ROWS)

    def block_rows(index):
        return slice(index * block, (index + 1) * block)

    for index in range(count):
        back_ref[block_rows(index), :] = lax.dot_general(
            grad_ref[block_rows(index), :],
            proj_ref[...],
            (((1,), (1,)), ((), ())),
            preferred_element_type=wide,
        ).astype(jnp.bfloat16)

    def weigh(index):
        total = jnp.zeros((8, block), wide)
        for start in steps:
            keys = slice(start, start + KEY_ROWS)
            weight_grad = lax.dot_general(
                value_ref[keys, :],
                back_ref[block_rows(index), :],
                (((1,), (1,)), ((), ())),
                preferred_element_type=wide,
            )
            grads_refs[index][keys, :] = weight_grad
            total = total + fold(soft_ref[keys, block_rows(index)].astype(wide) * weight_grad)
        return column_total(total)

    def slope(index, dots):
        for start in steps:
            keys = slice(start, start + KEY_ROWS)
            weights = soft_ref[keys, block_rows(index)].astype(wide)
            score_grad_ref[keys, block_rows(index)] = (
                weights * (grads_refs[index][keys, :] - dots)
            ).astype(jnp.bfloat16)

    dots = weigh(0)
    for index in range(count):
        now, rows = dots, block_rows(index)
        if index + 1 < count:
            dots = weigh(index + 1)
        slope(index, now)
        packed_ref[rows, 2 * channels :] = jnp.dot(
            soft_ref[rows, :], back_ref[...], preferred_element_type=wide
        ).astype(jnp.bfloat16)
        query_grad = jnp.dot(
            key_flip_ref[...], score_grad_ref[:, rows], preferred_element_type=wide
        )
        packed_ref[rows, 0:channels] = (query_grad * score_scale).astype(jnp.bfloat16).T
    for index in range(count):
        rows = block_rows(index)
        packed_ref[rows, channels : 2 * channels] = (
            jnp.dot(score_grad_ref[rows, :], query_ref[...], preferred_element_type=wide)
            * score_scale
        ).astype(jnp.bfloat16)

    def pack(rows, carry):
        return (
            carry[0] + fold(packed_ref[rows, 0:channels].astype(wide)),
            carry[1] + fold(packed_ref[rows, 2 * channels :].astype(wide)),
            carry[2] + fold(grad_ref[rows, :].astype(wide)),
        )

    zeros = jnp.zeros((8, channels), wide)
    totals = zeros, zeros, zeros
    for start in range(0, pixels, CHUNK):
        totals = pack(pl.ds(start, CHUNK), totals)
    sums_ref[...] = jnp.zeros(sums_ref.shape, wide)
    for row, total in enumerate(totals):
        sums_ref[8 + row : 9 + row, :] = column_total(total)
    mixed_ref[:, 0 : 3 * channels] = jnp.dot(
        flip_ref[...], packed_ref[...], preferred_element_type=wide
    ).astype(jnp.bfloat16)
    mixed_ref[:, 3 * channels :] = jnp.dot(
        out_flip_ref[own, :], grad_ref[...], preferred_element_type=wide
    ).astype(jnp.bfloat16)
    keep_half(mixed_ref, 0, keep_ref, send_ref)


def third_kernel(
    qkv_ref,
    grad_ref,
    packed_ref,
    residual_ref,
    table_ref,
    act_two_ref,
    lanes_ref,
    old_sums_ref,
    residual_grad_ref,
    grad_two_ref,
    sums_ref,
    part_ref,
    total_ref,
    flip_ref,
    columns_ref,
    *,
    cols,
):
    pixels, channels = residual_ref.shape
    block = FILL_ROWS
    wide = jnp.float32
    mean, inverse, gain, shift = norm_rows(table_ref, 2)
    zeros = jnp.zeros((8, channels), wide)

    sums = (zeros, zeros)
    for start in range(0, pixels, block):
        rows = pl.ds(start, block)
        normed_grad = lax.dot_general(
            packed_ref[rows, :], qkv_ref[...], (((1,), (1,)), ((), ())), preferred_element_type=wide
        )
        total_ref[rows, :] = normed_grad
        centered = residual_ref[rows, :] - mean
        sums = sums[0] + fold(normed_grad), sums[1] + fold(normed_grad * centered)
    sums = sums[0], sums[1] * inverse
    sums_ref[...] = old_sums_ref[...]
    sums_ref[5:6, :] = column_total(sums[1])
    sums_ref[6:7, :] = column_total(sums[0])
    back = norm_back(
        total_ref, False, sums, lambda rows: residual_ref[rows, :], table_ref, 2, pixels
    )

    def finish(rows, carry):
        total = grad_ref[rows, :].astype(wide) + back(rows, rows)
        residual_grad_ref[rows, :] = total
        low = total.astype(jnp.bfloat16)
        grad_two_ref[rows, :] = low
        return carry + fold(low.astype(wide))

    sums_ref[7:8, :] = column_total(each_chunk(pixels, finish, zeros))
    narrow = grad_two_ref[:, own_lanes()]
    weight_part(act_two_ref, narrow, lanes_ref, flip_ref, columns_ref, part_ref, cols)


def second_kernel(
    old_total_ref,
    taps_ref,
    middle_ref,
    table_ref,
    act_one_ref,
    mask_ref,
    lanes_ref,
    weights_ref,
    old_sums_ref,
    part_two_ref,
    grad_one_ref,
    sums_ref,
    keep_one_ref,
    send_one_ref,
    keep_two_ref,
    send_two_ref,
    total_ref,
    flip_ref,
    columns_ref,
    part_ref,
    scales_ref,
    *,
    cols,
):
    pixels, channels = middle_ref.shape

    def read(rows):
        return middle_ref[rows, :]

    sums = finish_back(
        weights_ref.at[1], mask_ref, taps_ref, total_ref, read, table_ref, 1, cols, old_total_ref
    )
    back = norm_back(total_ref, True, sums, read, table_ref, 1, pixels, scales_ref)
    narrow = narrow_back(total_ref, middle_ref, scales_ref).astype(jnp.bfloat16)
    weight_part(act_one_ref, narrow, lanes_ref, flip_ref, columns_ref, part_ref, cols)
    sums_ref[...] = old_sums_ref[...]
    sums_ref[2:3, :] = column_total(sums[1])
    sums_ref[3:4, :] = column_total(sums[0])

    def finish(rows, carry):
        low = back(rows, rows).astype(jnp.bfloat16)
        grad_one_ref[rows, :] = low
        return carry + fold(low.astype(jnp.float32))

    zeros = jnp.zeros((8, channels), jnp.float32)
    sums_ref[4:5, :] = column_total(each_chunk(pixels, finish, zeros))
    keep_half(part_ref, 1, keep_one_ref, send_one_ref)
    keep_half(part_two_ref, 1, keep_two_ref, send_two_ref)


def near_far():
    core = lax.axis_index("height") & 1
    return 1 + core, 2 - core


def keep_half(source_ref, axis, keep_ref, send_ref):
    me = lax.axis_index("canvas")
    near, far = near_far()
    rows, width = keep_ref.shape[0] // 2, keep_ref.shape[1]
    for target_ref, flip in ((keep_ref, 0), (send_ref, near)):
        for slot, other in enumerate((0, far)):
            owner = me ^ flip ^ other
            target = target_ref.at[slot * rows : (slot + 1) * rows, :]
            if axis == 0:
                target[...] = source_ref[pl.ds(pl.multiple_of(owner * rows, rows), rows), :]
            else:
                target[...] = source_ref[:, pl.ds(pl.multiple_of(owner * width, width), width)]


def first_kernel(
    grad_one_ref,
    features_ref,
    table_ref,
    mask_ref,
    old_sums_ref,
    weights_ref,
    own_ref,
    sums_ref,
    partial_ref,
    total_ref,
    taps_ref,
    *,
    cols,
):
    def read(rows):
        return features_ref[rows, :].astype(jnp.float32)

    weights = weights_ref.at[0]
    begin_back(grad_one_ref, weights, mask_ref, taps_ref, total_ref, cols)
    sums = finish_back(weights, mask_ref, taps_ref, total_ref, read, table_ref, 0, cols)
    partial_ref[0:8, :], partial_ref[8:16, :] = sums
    sums_ref[...] = old_sums_ref[...]
    sums_ref[0:1, :] = column_total(sums[1])
    sums_ref[1:2, :] = column_total(sums[0])
    count = own_ref.shape[0]
    own = pl.ds(pl.multiple_of(lax.axis_index("height") * count, count), count)
    own_ref[...] = total_ref[own, :]


def own_kernel(
    own_ref, partial_ref, features_ref, residual_grad_ref, table_ref, input_grad_ref
):
    def read(rows):
        return features_ref[rows, :].astype(jnp.float32)

    sums = partial_ref[0:8, :], partial_ref[8:16, :]
    pixels = features_ref.shape[0]
    back = norm_back(own_ref, True, sums, read, table_ref, 0, pixels)
    count = own_ref.shape[0]
    own = pl.ds(pl.multiple_of(lax.axis_index("height") * count, count), count)
    total = residual_grad_ref[own, :] + back(own, slice(0, count))
    input_grad_ref[...] = total.astype(jnp.bfloat16)


def place_kernel(*refs):
    joints, packed_ref = refs[:-1], refs[-1]
    share = packed_ref.shape[0] // len(joints)
    me = lax.axis_index("canvas")
    for step, joint in enumerate(joints):
        place = pl.ds(pl.multiple_of((me ^ step) * share, share), share)
        packed_ref[place, :] = joint[...]


def cut_kernel(packed_ref, *half_refs):
    rows = half_refs[0].shape[0]
    for index, half_ref in enumerate(half_refs):
        half_ref[...] = packed_ref[index * rows : (index + 1) * rows, :]


def spread_quarters(packed, flips, qkv_ref, proj_ref, qkv_hbm, proj_hbm, sems):
    quarter = packed[0].shape[0]
    inner = qkv_ref.shape[2]
    copies = []
    for index, packed_ref in enumerate(packed):
        owner = own_quarter() ^ flips[index]
        rows = pl.ds(pl.multiple_of(owner * quarter, quarter), quarter)
        qkv_ref[index] = packed_ref[:, 0:inner].astype(jnp.float32)
        proj_ref[index] = packed_ref[:, inner:].astype(jnp.float32)
        for which, (held, target) in enumerate(((qkv_ref, qkv_hbm), (proj_ref, proj_hbm))):
            copy = pltpu.make_async_copy(held.at[index], target.at[rows, :], sems.at[index, which])
            copy.start()
            copies.append(copy)
    return copies


def join_kernel(*refs):
    packed, (qkv_hbm, proj_hbm, qkv_ref, proj_ref, sems) = refs[:-5], refs[-5:]
    copies = spread_quarters(packed, [0, 2], qkv_ref, proj_ref, qkv_hbm, proj_hbm, sems)
    for copy in copies:
        copy.wait()


def halve_kernel(keep_ref, got_ref, hold_ref, send_ref):
    total = keep_ref[...].astype(jnp.float32) + got_ref[...].astype(jnp.float32)
    rows = hold_ref.shape[0]
    hold_ref[...] = total[0:rows]
    send_ref[0:rows, :] = total[rows:].astype(jnp.bfloat16)


def halve_both_kernel(
    keep_ref, got_ref, keep_two_ref, got_two_ref, hold_ref, send_ref, hold_two_ref
):
    rows = hold_ref.shape[0]
    halve_kernel(keep_ref, got_ref, hold_ref, send_ref)
    halve_kernel(keep_two_ref, got_two_ref, hold_two_ref, send_ref.at[rows : 2 * rows, :])


def last_kernel(
    chip_ref,
    both_a_ref,
    both_b_ref,
    old_qkv,
    old_proj,
    qkv_hbm,
    proj_hbm,
    qkv_ref,
    proj_ref,
    sems,
):
    copies = []
    rows = both_a_ref.shape[0]
    inner = qkv_ref.shape[2]
    chips = (chip_ref.at[0:rows, :], chip_ref.at[rows : 2 * rows, :])
    for index, piece_ref in enumerate((*chips, both_a_ref, both_b_ref)):
        start = ((own_quarter() ^ (1 if index < 2 else 3)) * 2 + index % 2) * rows
        target = pl.ds(pl.multiple_of(start, rows), rows)
        qkv_ref[index] = piece_ref[:, 0:inner].astype(jnp.float32)
        proj_ref[index] = piece_ref[:, inner:].astype(jnp.float32)
        for which, (held, whole) in enumerate(((qkv_ref, qkv_hbm), (proj_ref, proj_hbm))):
            copy = pltpu.make_async_copy(held.at[index], whole.at[target, :], sems.at[index, which])
            copy.start()
            copies.append(copy)
    for copy in copies:
        copy.wait()


def sums_kernel(
    sums_ref,
    got_sums_ref,
    hold_one_ref,
    hold_two_ref,
    got_ref,
    share_ref,
    gains_ref,
    shifts_ref,
    conv_ref,
    qv_ref,
    bias_ref,
):
    rows = hold_one_ref.shape[0]
    for which, hold_ref in enumerate((hold_one_ref, hold_two_ref)):
        got = got_ref[which * rows : (which + 1) * rows, :].astype(jnp.float32)
        share_ref[which] = (hold_ref[...] + got).reshape(share_ref.shape[1:])
    total = sums_ref[...] + got_sums_ref[...]
    for row, start in enumerate((0, 2, 5)):
        gains_ref[row : row + 1, :] = total[start : start + 1]
        shifts_ref[row : row + 1, :] = total[start + 1 : start + 2]
    conv_ref[0:1, :] = total[4:5]
    conv_ref[1:2, :] = total[7:8]
    qv_ref[...] = total[8:10]
    bias_ref[...] = total[10:11]


def call_kernel(kernel, outputs, scratch, operands, places, flops, limit, out_places=None, aliases={}):
    out_places = out_places or "v" * len(outputs)
    spaces = {
        "v": pl.BlockSpec(memory_space=pltpu.VMEM),
        "s": pl.BlockSpec(memory_space=pltpu.SMEM),
        "h": pl.BlockSpec(memory_space=pl.ANY),
        "o": pl.BlockSpec(memory_space=pltpu.VMEM),
        "a": pl.BlockSpec(memory_space=pl.ANY),
    }
    moved = 8 * flops // LANES
    held = {"v": pltpu.VMEM, "h": pltpu.HBM, "o": jax.ShapeDtypeStruct}
    operands = [
        pltpu.with_memory_space_constraint(array, pltpu.HBM) if place == "h" else array
        for array, place in zip(operands, places)
    ]
    return pl.pallas_call(
        kernel,
        out_shape=[held[place](*output) for output, place in zip(outputs, out_places)],
        in_specs=[spaces[place] for place in places],
        out_specs=[spaces[place] for place in out_places],
        scratch_shapes=scratch,
        input_output_aliases=aliases,
        compiler_params=pltpu.CompilerParams(vmem_limit_bytes=limit * 2**20),
        cost_estimate=pl.CostEstimate(flops=flops, bytes_accessed=moved, transcendentals=0),
    )(*operands)


def send_height(block, step):
    size = lax.axis_size("height")
    return lax.ppermute(block, "height", [(i, i ^ step) for i in range(size)])


def with_cores(blocks, other):
    pieces = [blocks[0], other]
    for block in blocks[1:]:
        pieces += [block, send_height(block, 1)]
    return pieces


def send_canvas(block, step):
    size = lax.axis_size("canvas")
    return lax.ppermute(block, "canvas", [(i, i ^ step) for i in range(size)])


def send_phase(block, phase):
    canvases, size = lax.axis_size("canvas"), lax.axis_size("height")
    pairs = []
    for canvas in range(canvases):
        for height in range(size):
            step = 2 if (height ^ phase) & 1 else 1
            pairs.append((canvas * size + height, (canvas ^ step) * size + height))
    return lax.ppermute(block, ("canvas", "height"), pairs)


def trade_canvas(pieces):
    return [pieces[0]] + [send_canvas(piece, step) for step, piece in enumerate(pieces) if step]


def whole_canvas(
    features,
    tile_ids,
    norm_gains,
    norm_shifts,
    conv_weights,
    conv_biases,
    qkv_weight,
    qv_bias,
    proj_weight,
    proj_bias,
    cotangent,
):
    height_size = lax.axis_size("height")
    canvas_size = lax.axis_size("canvas")
    local_rows, cols, channels = features.shape[1:]
    all_rows = tile_ids.shape[1]
    pixels = all_rows * cols
    own_pixels = local_rows * cols
    out_share = channels // height_size
    ci_share = channels // canvas_size
    quarter = channels // 4
    row_share = quarter // canvas_size
    low, wide = jnp.bfloat16, jnp.float32

    own_features = features.reshape(own_pixels, channels)
    own_grad = cotangent.reshape(own_pixels, channels)
    steps = range(2, height_size, 2)
    held_features = [own_features] + [send_height(own_features, step) for step in steps]
    plane = ((pixels, channels), low)
    plane_wide = ((pixels, channels), wide)
    sums_shape = ((16, channels), wide)
    mixed_halves = [((2 * row_share, 4 * channels), low)] * 2
    taps = pltpu.VMEM((pixels + 2 * cols, 3 * channels), low)
    held_wide = pltpu.VMEM((pixels, channels), wide)
    flipped = pltpu.VMEM((channels, pixels), low)
    narrow = pltpu.VMEM((NARROW, pixels), low)
    columns = pltpu.VMEM((9 * out_share, pixels), low)
    part_held = pltpu.VMEM((9 * out_share, channels), low)
    sem = pltpu.SemaphoreType.DMA
    conv_flops = 2 * 9 * pixels * channels * channels
    dot_flops = 2 * pixels * channels * channels
    score_flops = 2 * pixels * pixels * channels
    scale = channels ** (-0.5)

    (
        held_conv,
        turned,
        held_qkv,
        held_proj,
        params,
        mask,
        lane_mask,
        id_rows,
        id_cols,
    ) = call_kernel(
        functools.partial(hold_kernel, cols=cols),
        [
            (conv_weights.shape, low),
            ((2, 3, channels, 3 * channels), low),
            (qkv_weight.shape, low),
            (proj_weight.shape, low),
            ((24, channels), wide),
            ((2, pixels, LANES), wide),
            ((8, pixels), wide),
            ((pixels, LANES), jnp.int32),
            ((8, pixels), jnp.int32),
        ],
        [
            pltpu.SMEM(tile_ids.shape, jnp.int32),
            pltpu.VMEM(norm_gains.shape, wide),
            pltpu.VMEM(norm_shifts.shape, wide),
            pltpu.VMEM(conv_biases.shape, wide),
            pltpu.VMEM(qv_bias.shape, wide),
            pltpu.VMEM((1, channels), wide),
            sem((27,)),
        ],
        [
            tile_ids,
            norm_gains,
            norm_shifts,
            conv_biases,
            conv_weights,
            qkv_weight,
            proj_weight,
            qv_bias,
            proj_bias.reshape(1, channels),
        ],
        "h" * 9,
        conv_flops,
        8,
    )
    held_features[1:] = [
        lax.optimization_barrier((params, block))[1] for block in held_features[1:]
    ]
    other_core = send_height(jnp.concatenate([own_features, own_grad], axis=0), 1)
    pieces = with_cores(held_features, other_core)
    far_grad, *pieces[4::2] = lax.optimization_barrier((own_grad, *held_features[2:]))
    held_grads = [own_grad, send_height(own_grad, 2)]
    held_grads[1], pieces[2] = lax.optimization_barrier((held_grads[1], held_features[1]))
    held_grads += [send_height(far_grad, step) for step in steps[1:]]

    all_features, act_one, middle, act_two, residual, table = call_kernel(
        functools.partial(conv_kernel, cols=cols, count=height_size),
        [plane, plane, plane_wide, plane, plane_wide, ((24, channels), wide)],
        [pltpu.VMEM((own_pixels, channels), low), taps, sem],
        [*pieces, held_conv, params, mask],
        "h" + "v" * (height_size + 2),
        2 * conv_flops,
        16,
    )
    residual, *held_grads = lax.optimization_barrier((residual, *held_grads))
    grad_pieces = with_cores(held_grads, other_core)
    normed, query, key, value, soft, out_flip, output = call_kernel(
        functools.partial(score_kernel, score_scale=scale),
        [
            plane,
            plane,
            plane,
            plane,
            ((pixels, pixels), low),
            ((channels, pixels), low),
            ((own_pixels, channels), low),
        ],
        [
            flipped,
            *[pltpu.VMEM((pixels, SCORE_ROWS), wide)] * (pixels // SCORE_ROWS),
        ],
        [
            held_qkv,
            held_proj,
            residual,
            table,
            id_rows,
            id_cols,
        ],
        "vvvvvv",
        3 * dot_flops + 2 * score_flops,
        20,
        "v" * 6 + "o",
    )
    normed, *grad_pieces = lax.optimization_barrier((normed, *grad_pieces))
    all_grad, packed, sums, keep_mixed, send_mixed = call_kernel(
        functools.partial(attention_kernel, score_scale=scale, count=height_size),
        [plane, ((pixels, 3 * channels), low), sums_shape, *mixed_halves],
        [
            pltpu.VMEM((quarter, 4 * channels), low),
            flipped,
            pltpu.VMEM((pixels, channels), low),
            pltpu.VMEM((pixels, pixels), low),
            pltpu.VMEM((quarter, pixels), low),
            sem((height_size,)),
            *[pltpu.VMEM((pixels, SCORE_ROWS), wide)] * (pixels // SCORE_ROWS),
        ],
        [held_proj, normed, query, key, value, soft, out_flip, *grad_pieces],
        "vvvvvvvh" + "a" * (height_size - 1),
        3 * dot_flops + 4 * score_flops,
        20,
    )
    got_mixed = send_phase(send_mixed, 0)
    residual_grad, grad_two, sums, part_two = call_kernel(
        functools.partial(third_kernel, cols=cols),
        [plane_wide, plane, sums_shape, ((9 * out_share, channels), low)],
        [held_wide, narrow, columns],
        [held_qkv, all_grad, packed, residual, table, act_two, lane_mask, sums],
        "vvvvvvvv",
        3 * dot_flops + conv_flops // height_size,
        16,
    )
    grad_two, got_mixed = lax.optimization_barrier((grad_two, got_mixed))
    hold_mixed, send_mixed = call_kernel(
        halve_kernel,
        [((row_share, 4 * channels), kind) for kind in (wide, low)],
        [],
        [keep_mixed, got_mixed],
        "vv",
        1,
        12,
    )
    got_mixed = send_phase(send_mixed, 1)
    grad_two, hold_mixed = lax.optimization_barrier((grad_two, hold_mixed))
    half_total, half_taps = call_kernel(
        functools.partial(turn_kernel, cols=cols),
        [plane_wide, (taps.shape, low)],
        [],
        [grad_two, mask, turned],
        "vvv",
        2 * conv_flops // 3,
        16,
    )
    half_total, got_mixed = lax.optimization_barrier((half_total, got_mixed))
    mixed_sum = (hold_mixed + got_mixed.astype(wide)).astype(low)
    joints = trade_canvas([mixed_sum] * canvas_size)
    halves = [((2 * 9 * out_share, ci_share), low)] * 4
    grad_one, sums, keep_one, send_one, keep_two, send_two = call_kernel(
        functools.partial(second_kernel, cols=cols),
        [plane, sums_shape, *halves],
        [held_wide, narrow, columns, part_held, pltpu.VMEM((8, channels), wide)],
        [half_total, half_taps, middle, table, act_one, mask, lane_mask, turned, sums, part_two],
        "v" * 10,
        conv_flops // 2,
        20,
    )
    grad_one, *joints = lax.optimization_barrier((grad_one, *joints))
    (own_mixed,) = call_kernel(
        place_kernel,
        [((quarter, 4 * channels), low)],
        [],
        joints,
        "v" * canvas_size,
        1,
        12,
    )
    own_mixed, send_one, send_two = lax.optimization_barrier((own_mixed, send_one, send_two))
    chip_mixed = send_height(own_mixed, 2)
    core_mixed = send_height(own_mixed, 1)
    got_one, got_two = send_phase(send_one, 0), send_phase(send_two, 0)
    own_total, sums, partial_sums = call_kernel(
        functools.partial(first_kernel, cols=cols),
        [((own_pixels, channels), wide), sums_shape, sums_shape],
        [held_wide, taps],
        [grad_one, all_features, table, mask, sums, turned],
        "vvvvvv",
        1,
        20,
    )
    got_sums, own_sums = send_phase(sums, 0), sums
    sums, core_mixed, got_one, got_two = lax.optimization_barrier(
        (sums, core_mixed, got_one, got_two)
    )
    share_rows = 9 * out_share
    hold_one, send_share, hold_two = call_kernel(
        halve_both_kernel,
        [
            ((share_rows, ci_share), wide),
            ((2 * share_rows, ci_share), low),
            ((share_rows, ci_share), wide),
        ],
        [],
        [keep_one, got_one, keep_two, got_two],
        "vvvv",
        1,
        12,
    )
    got_share = send_phase(send_share, 1)

    def widened(count, rows):
        return [
            pltpu.VMEM((count, rows, 3 * channels), wide),
            pltpu.VMEM((count, rows, channels), wide),
            sem((count, 2)),
        ]

    grad_shapes = [(qkv_weight.shape, wide), (proj_weight.shape, wide)]
    core_mixed, hold_one = lax.optimization_barrier((core_mixed, hold_one))
    qkv_grad, proj_grad = call_kernel(
        join_kernel,
        grad_shapes,
        widened(2, quarter),
        [own_mixed, core_mixed],
        "vv",
        1,
        12,
        "hh",
    )
    qkv_grad, chip_mixed, got_sums = lax.optimization_barrier((qkv_grad, chip_mixed, got_sums))
    sums = own_sums + got_sums
    got_sums = send_phase(sums, 1)
    chip_halves = call_kernel(
        cut_kernel,
        [((quarter // 2, 4 * channels), low)] * 2,
        [],
        [chip_mixed],
        "v",
        1,
        12,
    )
    both_halves = [send_height(half, 1) for half in chip_halves]
    qkv_grad, proj_grad = call_kernel(
        last_kernel,
        grad_shapes,
        widened(4, quarter // 2),
        [chip_mixed, *both_halves, qkv_grad, proj_grad],
        "vvvhh",
        1,
        12,
        "hh",
        {3: 0, 4: 1},
    )
    qkv_grad, own_total = lax.optimization_barrier((qkv_grad, own_total))
    (input_grad,) = call_kernel(
        own_kernel,
        [((own_pixels, channels), low)],
        [],
        [own_total, partial_sums, all_features, residual_grad, table],
        "vvvvv",
        dot_flops // 4,
        12,
        "o",
    )
    input_grad, got_share, got_sums = lax.optimization_barrier((input_grad, got_share, got_sums))
    vector_shapes = [norm_gains.shape, norm_shifts.shape, conv_biases.shape, qv_bias.shape]
    conv_grad, gains_grad, shifts_grad, biases_grad, qv_grad, proj_bias_grad = call_kernel(
        sums_kernel,
        [((2, 3, 3, out_share, ci_share), wide)]
        + [(shape, wide) for shape in vector_shapes + [(1, channels)]],
        [],
        [sums, got_sums, hold_one, hold_two, got_share],
        "vvvvv",
        1,
        12,
        "o" * 6,
    )
    own_shape = (1, local_rows, cols, channels)
    return (
        output.reshape(own_shape),
        input_grad.reshape(own_shape),
        gains_grad,
        shifts_grad,
        jnp.swapaxes(conv_grad, 3, 4),
        biases_grad,
        qkv_grad,
        qv_grad,
        proj_grad,
        proj_bias_grad.reshape(channels),
    )


def on_device(*arrays):
    features, tile_ids = arrays[0], arrays[1]
    local_rows, cols, channels = features.shape[1:]
    pixels = tile_ids.shape[1] * cols
    height_size, canvas_size = lax.axis_size("height"), lax.axis_size("canvas")
    powers = all(size & (size - 1) == 0 for size in (height_size, canvas_size, cols))
    fits = (
        powers
        and height_size > 2
        and canvas_size == 4
        and channels == LANES * canvas_size
        and pixels <= MOST_PIXELS
        and pixels % FILL_ROWS == 0
        and FILL_ROWS % CHUNK == 0
        and pixels % SCORE_ROWS == 0
        and pixels % KEY_ROWS == 0
        and (local_rows * cols) % LANES == 0
        and CHUNK % cols == 0
        and cols % 16 == 0
        and channels % (LANES * canvas_size) == 0
        and 2 * channels == NARROW * height_size
    )
    return whole_canvas(*arrays) if fits else split_canvas(*arrays)


def solution(mesh):
    in_specs = (
        P("canvas", "height", None, None),
        P("canvas", None),
        P(),
        P(),
        P(),
        P(),
        P(),
        P(),
        P(),
        P(),
        P("canvas", "height", None, None),
    )
    out_specs = (
        P("canvas", "height", None, None),
        P("canvas", "height", None, None),
        P(),
        P(),
        P(None, None, None, "canvas", "height"),
        P(),
        P(),
        P(),
        P(),
        P(),
    )
    return jax.shard_map(
        on_device, mesh=mesh, in_specs=in_specs, out_specs=out_specs, check_vma=False
    )
```

```python
import functools

import jax
import jax.numpy as jnp
from jax import lax
from jax.experimental import pallas as pl
from jax.experimental.pallas import tpu as pltpu
from jax.sharding import PartitionSpec as P

GROUPS = 32


epsilon = 1e-06
masked_score = -1e30
MOST_PIXELS = 1024
LANES = 128
NARROW = 128
CHUNK = 128
FILL_ROWS = 256
QUERY_ROWS = 512
SCORE_ROWS = 256
KEY_ROWS = 256


def extended(block, sides, width):
    for axis, dim in sides:
        count = lax.axis_size(axis)
        forward = [(i, i + 1) for i in range(count - 1)]
        backward = [(target, source) for source, target in forward]
        low = lax.ppermute(
            lax.slice_in_dim(block, block.shape[dim] - width, None, axis=dim), axis, forward
        )
        high = lax.ppermute(lax.slice_in_dim(block, 0, width, axis=dim), axis, backward)
        block = jnp.concatenate([low, block, high], axis=dim)
    return block


def group_total(vector):
    return vector.reshape(GROUPS, -1).sum(axis=1)


def spread_groups(vector, channels):
    return jnp.repeat(vector, channels // GROUPS)


def norm_forward(values, gain, shift, members):
    channels = values.shape[1]
    totals = lax.psum(group_total(jnp.sum(values, axis=0)), "height")
    centered = values - spread_groups(totals / members, channels)
    squares = lax.psum(group_total(jnp.sum(centered * centered, axis=0)), "height")
    inverse = spread_groups(lax.rsqrt(squares / members + epsilon), channels)
    normed = centered * inverse
    return (normed, inverse, normed * gain + shift)


def norm_backward(grad_in, normed, inverse, gain, members):
    channels = grad_in.shape[1]
    scaled = grad_in * gain
    both_sums = lax.psum(
        (group_total(jnp.sum(scaled, axis=0)), group_total(jnp.sum(scaled * normed, axis=0))),
        "height",
    )
    mean_grad = spread_groups(both_sums[0] / members, channels)
    mean_cross = spread_groups(both_sums[1] / members, channels)
    result = inverse * (scaled - mean_grad - normed * mean_cross)
    return (result, jnp.sum(grad_in * normed, axis=0), jnp.sum(grad_in, axis=0))


def swish(values):
    return values * jax.nn.sigmoid(values)


def swish_slope(values):
    sigmoid_part = jax.nn.sigmoid(values)
    return sigmoid_part * (1.0 + values * (1.0 - sigmoid_part))


def tap_columns(padded, row_mask, local_rows, canvas_cols):
    pieces = []
    for row_tap in range(3):
        rows_taken = padded[row_tap : row_tap + local_rows] * row_mask[:, row_tap, None, None]
        for col_tap in range(3):
            pieces.append(rows_taken[:, col_tap : col_tap + canvas_cols])
    stacked = jnp.concatenate(pieces, axis=2)
    return stacked.reshape(local_rows * canvas_cols, stacked.shape[2])


def conv_forward(acts, row_mask, weight, bias):
    local_rows, canvas_cols, channels = acts.shape
    rimmed = extended(acts, (("height", 0),), 1)
    padded = jnp.pad(rimmed, ((0, 0), (1, 1), (0, 0)))
    gathered = tap_columns(padded, row_mask, local_rows, canvas_cols)
    result = (
        jnp.dot(
            gathered, weight.reshape(9 * channels, channels), preferred_element_type=jnp.float32
        )
        + bias
    )
    return (result, gathered)


def conv_backward(grad_low, row_mask, weight, gathered):
    local_rows, canvas_cols, channels = grad_low.shape
    flat_grad = grad_low.reshape(local_rows * canvas_cols, channels)
    weight_grad = lax.dot_general(
        gathered, flat_grad, (((0,), (0,)), ((), ())), preferred_element_type=jnp.float32
    )
    rimmed = extended(grad_low, (("height", 0),), 1)
    padded = jnp.pad(rimmed, ((0, 0), (1, 1), (0, 0)))
    grad_taps = tap_columns(padded, row_mask, local_rows, canvas_cols)
    flipped = jnp.transpose(weight[::-1, ::-1], (0, 1, 3, 2)).reshape(9 * channels, channels)
    input_part = jnp.dot(grad_taps, flipped, preferred_element_type=jnp.float32)
    return (
        input_part,
        weight_grad.reshape(3, 3, channels, channels),
        jnp.sum(flat_grad.astype(jnp.float32), axis=0),
    )


def take_rows(array, offset, count):
    return lax.dynamic_slice_in_dim(array, offset, count)


def score_grads(
    queries, out_grad, log_total, row_dots, query_ids, key_rows, value_rows, key_ids, score_scale
):
    scores = (
        lax.dot_general(
            queries, key_rows, (((1,), (1,)), ((), ())), preferred_element_type=jnp.float32
        )
        * score_scale
    )
    same_tile = query_ids[:, None] == key_ids[None, :]
    softmax_block = jnp.exp(jnp.where(same_tile, scores - log_total[:, None], masked_score))
    weight_grad = lax.dot_general(
        out_grad, value_rows, (((1,), (1,)), ((), ())), preferred_element_type=jnp.float32
    )
    score_grad = (softmax_block * (weight_grad - row_dots[:, None])).astype(jnp.bfloat16)
    return (softmax_block.astype(jnp.bfloat16), score_grad)


def split_canvas(
    features,
    tile_ids,
    norm_gains,
    norm_shifts,
    conv_weights,
    conv_biases,
    qkv_weight,
    qv_bias,
    proj_weight,
    proj_bias,
    cotangent,
):
    height_size = lax.axis_size("height")
    local_rows = features.shape[1]
    canvas_cols = features.shape[2]
    channels = features.shape[3]
    pixels = local_rows * canvas_cols
    row_ids = tile_ids[0]
    all_rows = row_ids.shape[0]
    members = float(all_rows * canvas_cols * (channels // GROUPS))
    score_scale = channels ** (-0.5)
    first_row = lax.axis_index("height") * local_rows
    edge_ids = jnp.full((1,), -1, jnp.int32)
    padded_ids = jnp.concatenate([edge_ids, row_ids, edge_ids])
    near_ids = lax.dynamic_slice_in_dim(padded_ids, first_row, local_rows + 2)
    own_rows = near_ids[1 : local_rows + 1]
    row_mask = jnp.stack(
        [near_ids[row_tap : row_tap + local_rows] == own_rows for row_tap in range(3)], axis=1
    ).astype(jnp.bfloat16)
    key_ids = jnp.repeat(row_ids, canvas_cols)
    query_ids = jnp.repeat(own_rows, canvas_cols)
    grid_shape = (local_rows, canvas_cols, channels)
    inputs = features[0].reshape(pixels, channels).astype(jnp.float32)
    normed_one, inverse_one, pre_one = norm_forward(inputs, norm_gains[0], norm_shifts[0], members)
    act_one = swish(pre_one).astype(jnp.bfloat16).reshape(grid_shape)
    middle, taps_one = conv_forward(act_one, row_mask, conv_weights[0], conv_biases[0])
    normed_two, inverse_two, pre_two = norm_forward(middle, norm_gains[1], norm_shifts[1], members)
    act_two = swish(pre_two).astype(jnp.bfloat16).reshape(grid_shape)
    branch, taps_two = conv_forward(act_two, row_mask, conv_weights[1], conv_biases[1])
    residual = inputs + branch
    normed_three, inverse_three, pre_three = norm_forward(
        residual, norm_gains[2], norm_shifts[2], members
    )
    attn_input = pre_three.astype(jnp.bfloat16)
    mixed = jnp.dot(attn_input, qkv_weight, preferred_element_type=jnp.float32)
    queries = (mixed[:, :channels] + qv_bias[0]).astype(jnp.bfloat16)
    key_rows = mixed[:, channels : 2 * channels].astype(jnp.bfloat16)
    value_rows = (mixed[:, 2 * channels :] + qv_bias[1]).astype(jnp.bfloat16)
    running_max = jnp.full((pixels,), masked_score, jnp.float32)
    key_piece = lax.all_gather(key_rows, "height", axis=0, tiled=True)
    value_piece = lax.all_gather(value_rows, "height", axis=0, tiled=True)
    scores = (
        lax.dot_general(
            queries, key_piece, (((1,), (1,)), ((), ())), preferred_element_type=jnp.float32
        )
        * score_scale
    )
    same_tile = query_ids[:, None] == key_ids[None, :]
    scores = jnp.where(same_tile, scores, masked_score)
    new_max = jnp.maximum(running_max, jnp.max(scores, axis=1))
    weights = jnp.where(same_tile, jnp.exp(scores - new_max[:, None]), 0.0)
    summed_out = jnp.dot(
        weights.astype(jnp.bfloat16), value_piece, preferred_element_type=jnp.float32
    )
    total_weight = jnp.sum(weights, axis=1)
    log_total = new_max + jnp.log(total_weight)
    attended = summed_out / total_weight[:, None]
    attended_low = attended.astype(jnp.bfloat16)
    output = (
        residual
        + jnp.dot(attended_low, proj_weight, preferred_element_type=jnp.float32)
        + proj_bias
    )
    out_grad = cotangent[0].reshape(pixels, channels)
    out_grad_full = out_grad.astype(jnp.float32)
    proj_grad = lax.dot_general(
        attended_low, out_grad, (((0,), (0,)), ((), ())), preferred_element_type=jnp.float32
    )
    proj_bias_grad = jnp.sum(out_grad_full, axis=0)
    attended_grad = lax.dot_general(
        out_grad, proj_weight, (((1,), (1,)), ((), ())), preferred_element_type=jnp.float32
    ).astype(jnp.bfloat16)
    row_dots = jnp.sum(attended_grad.astype(jnp.float32) * attended, axis=1)
    block_rows = pixels * min(height_size, 8)
    zero_block = jnp.zeros((pixels, channels), jnp.float32)
    key_all, value_all = (
        lax.all_gather(key_rows, "height", axis=0, tiled=True),
        lax.all_gather(value_rows, "height", axis=0, tiled=True),
    )
    query_all, grad_all = (
        lax.all_gather(queries, "height", axis=0, tiled=True),
        lax.all_gather(attended_grad, "height", axis=0, tiled=True),
    )
    total_all, dots_all = (
        lax.all_gather(log_total, "height", axis=0, tiled=True),
        lax.all_gather(row_dots, "height", axis=0, tiled=True),
    )

    def own_query_step(running, block_index):
        offset = block_index * block_rows
        key_part = take_rows(key_all, offset, block_rows)
        rounded, score_grad = score_grads(
            queries,
            attended_grad,
            log_total,
            row_dots,
            query_ids,
            key_part,
            take_rows(value_all, offset, block_rows),
            take_rows(key_ids, offset, block_rows),
            score_scale,
        )
        return (
            running
            + jnp.dot(score_grad, key_part, preferred_element_type=jnp.float32) * score_scale,
            None,
        )

    def own_key_step(running, block_index):
        offset = block_index * block_rows
        query_part = take_rows(query_all, offset, block_rows)
        grad_part = take_rows(grad_all, offset, block_rows)
        rounded, score_grad = score_grads(
            query_part,
            grad_part,
            take_rows(total_all, offset, block_rows),
            take_rows(dots_all, offset, block_rows),
            take_rows(key_ids, offset, block_rows),
            key_rows,
            value_rows,
            query_ids,
            score_scale,
        )
        key_part = (
            lax.dot_general(
                score_grad, query_part, (((0,), (0,)), ((), ())), preferred_element_type=jnp.float32
            )
            * score_scale
        )
        value_part = lax.dot_general(
            rounded, grad_part, (((0,), (0,)), ((), ())), preferred_element_type=jnp.float32
        )
        return ((running[0] + key_part, running[1] + value_part), None)

    block_count = key_all.shape[0] // block_rows
    query_grad, unused_one = lax.scan(own_query_step, zero_block, jnp.arange(block_count))
    (key_grad, value_grad), unused_two = lax.scan(
        own_key_step, (zero_block, zero_block), jnp.arange(block_count)
    )
    query_low = query_grad.astype(jnp.bfloat16)
    key_low = key_grad.astype(jnp.bfloat16)
    value_low = value_grad.astype(jnp.bfloat16)
    stacked_grad = jnp.concatenate([query_low, key_low, value_low], axis=1)
    qkv_grad = lax.dot_general(
        attn_input, stacked_grad, (((0,), (0,)), ((), ())), preferred_element_type=jnp.float32
    )
    qv_grad = jnp.stack(
        [
            jnp.sum(query_low.astype(jnp.float32), axis=0),
            jnp.sum(value_low.astype(jnp.float32), axis=0),
        ]
    )
    normed_grad = lax.dot_general(
        stacked_grad, qkv_weight, (((1,), (1,)), ((), ())), preferred_element_type=jnp.float32
    )
    back_three, gain_three, shift_three = norm_backward(
        normed_grad, normed_three, inverse_three, norm_gains[2], members
    )
    residual_grad = out_grad_full + back_three
    grad_two = residual_grad.astype(jnp.bfloat16).reshape(grid_shape)
    act_two_grad, weight_two_grad, bias_two_grad = conv_backward(
        grad_two, row_mask, conv_weights[1], taps_two
    )
    middle_grad, gain_two, shift_two = norm_backward(
        act_two_grad * swish_slope(pre_two), normed_two, inverse_two, norm_gains[1], members
    )
    grad_one = middle_grad.astype(jnp.bfloat16).reshape(grid_shape)
    act_one_grad, weight_one_grad, bias_one_grad = conv_backward(
        grad_one, row_mask, conv_weights[0], taps_one
    )
    input_back, gain_one, shift_one = norm_backward(
        act_one_grad * swish_slope(pre_one), normed_one, inverse_one, norm_gains[0], members
    )
    input_grad = residual_grad + input_back
    conv_grad = jnp.stack([weight_one_grad, weight_two_grad])
    conv_part = lax.psum_scatter(conv_grad, "height", scatter_dimension=4, tiled=True)
    conv_part = lax.psum_scatter(
        conv_part.astype(jnp.bfloat16), "canvas", scatter_dimension=3, tiled=True
    ).astype(jnp.float32)
    summed = lax.psum(
        (
            jnp.stack([gain_one, gain_two, gain_three]),
            jnp.stack([shift_one, shift_two, shift_three]),
            jnp.stack([bias_one_grad, bias_two_grad]),
            qkv_grad,
            qv_grad,
            proj_grad,
            proj_bias_grad,
        ),
        ("canvas", "height"),
    )
    return (
        output.astype(jnp.bfloat16).reshape((1,) + grid_shape),
        input_grad.astype(jnp.bfloat16).reshape((1,) + grid_shape),
        summed[0],
        summed[1],
        conv_part,
        summed[2],
        summed[3],
        summed[4],
        summed[5],
        summed[6],
    )


def fold(block):
    rows, width = block.shape
    return jnp.sum(block.reshape(rows // 8, 8, width), axis=0)


def group_lanes(block, group):
    lane = lax.broadcasted_iota(jnp.int32, block.shape, 1)
    width = block.shape[1]
    step = 1
    while step < group:
        above = pltpu.roll(block, step, 1)
        below = pltpu.roll(block, width - step, 1)
        block = block + jnp.where((lane & step) != 0, above, below)
        step *= 2
    return block


def group_mean(partial, members):
    spread = group_lanes(partial, partial.shape[1] // GROUPS)
    return jnp.sum(spread, axis=0, keepdims=True) * (1.0 / members)


def widen(block, width):
    return jnp.concatenate([block] * (width // block.shape[1]), axis=1)


def each_block(pixels, block, body, carry=0):
    def step(index, carry):
        return body(pl.ds(pl.multiple_of(index * block, block), block), carry)

    return lax.fori_loop(0, pixels // block, step, carry)


def each_chunk(pixels, body, carry):
    return each_block(pixels, CHUNK, body, carry)


def aligned(start, step):
    return start if isinstance(start, int) else pl.multiple_of(start, step)


class RunningStats:
    def __init__(self, channels):
        self.width = channels // GROUPS
        self.reference = None
        self.sums = self.squares = jnp.zeros((8, channels), jnp.float32)

    def add(self, block):
        if self.reference is None:
            self.reference = group_mean(block[0:8], 8.0 * self.width)
        offset = block - self.reference
        self.sums = self.sums + fold(offset)
        self.squares = self.squares + fold(offset * offset)

    def finish(self, pixels):
        both = group_lanes(jnp.concatenate([self.sums, self.squares], axis=0), self.width)
        share = 1.0 / (pixels * self.width)
        offset = column_total(both[0:8]) * share
        variance = column_total(both[8:16]) * share - offset * offset
        return self.reference + offset, lax.rsqrt(jnp.maximum(variance, 0.0) + epsilon)


def put_taps(taps_ref, block, rows, cols):
    count, channels = block.shape
    place = lax.broadcasted_iota(jnp.int32, block.shape, 0) & (cols - 1)
    left = jnp.where(place == 0, 0.0, pltpu.roll(block, 1, 0))
    right = jnp.where(place == cols - 1, 0.0, pltpu.roll(block, count - 1, 0))
    inner = pl.ds(aligned(rows.start + cols, cols), count)
    taps_ref[inner, 0:channels] = left.astype(jnp.bfloat16)
    taps_ref[inner, channels : 2 * channels] = block.astype(jnp.bfloat16)
    taps_ref[inner, 2 * channels :] = right.astype(jnp.bfloat16)


def clear_edges(taps_ref, cols):
    edge = jnp.zeros((cols, taps_ref.shape[1]), taps_ref.dtype)
    taps_ref[0:cols, :] = edge
    taps_ref[taps_ref.shape[0] - cols :, :] = edge


def begin_conv(taps_ref, product, total_ref, fill, first, cols):
    for start in range(0, total_ref.shape[0], FILL_ROWS):
        for inner in range(start, start + FILL_ROWS, CHUNK):
            fill(pl.ds(inner, CHUNK))
        rows = pl.ds(start, FILL_ROWS)
        total_ref[rows, :] = first(rows, product(taps_ref, pl.ds(start + cols, FILL_ROWS), 1))


def add_rows(taps_ref, product, mask_ref, total_ref, row_tap, last, cols, old_ref=None):
    pixels, channels = total_ref.shape
    old_ref = total_ref if old_ref is None else old_ref

    def step(rows, shifted):
        part = product(taps_ref, shifted, row_tap)
        mask = widen(mask_ref[row_tap // 2, rows, :], channels)
        value = old_ref[rows, :] + mask * part
        total_ref[rows, :] = value if last is None else last(rows, value)

    block = pixels if last is None else FILL_ROWS
    for start in range(0, pixels, block):
        step(pl.ds(start, block), pl.ds(start + row_tap * cols, block))


def run_conv(taps_ref, product, mask_ref, total_ref, fill, first, last, cols):
    begin_conv(taps_ref, product, total_ref, fill, first, cols)
    add_rows(taps_ref, product, mask_ref, total_ref, 0, None, cols)
    add_rows(taps_ref, product, mask_ref, total_ref, 2, last, cols)


def product_forward(weight_ref):
    channels = weight_ref.shape[-1]

    def product(taps_ref, shifted, row_tap):
        return jnp.dot(
            taps_ref[shifted, :],
            weight_ref[row_tap].reshape(3 * channels, channels),
            preferred_element_type=jnp.float32,
        )

    return product


def product_backward(weight_ref):
    def product(taps_ref, shifted, row_tap):
        return lax.dot_general(
            taps_ref[shifted, :],
            weight_ref[row_tap],
            (((1,), (1,)), ((), ())),
            preferred_element_type=jnp.float32,
        )

    return product


def activation(read, mean, inverse, gain, shift, act_ref, taps_ref, cols):
    scale, offset = 0.5 * inverse * gain, 0.5 * shift

    def fill(rows):
        half = (read(rows) - mean) * scale + offset
        act = half * (1.0 + jnp.tanh(half))
        act_ref[rows, :] = act.astype(jnp.bfloat16)
        put_taps(taps_ref, act, rows, cols)

    return fill


def back_means(sums, gain, pixels):
    channels = gain.shape[1]
    members = float(pixels * (channels // GROUPS))
    return group_mean(sums[0] * gain, members), group_mean(sums[1] * gain, members)


def column_total(partial):
    return jnp.sum(partial, axis=0, keepdims=True)


def weight_part(act_ref, narrow, lanes_ref, flip_ref, columns_ref, part_ref, cols):
    pixels, channels = act_ref.shape
    height = lax.axis_index("height")
    share = NARROW // 2
    flip_ref[...] = narrow.T
    own = pl.ds(pl.multiple_of((height % 2) * share, share), share)
    grad = flip_ref[own, :].astype(jnp.float32)
    column = lax.broadcasted_iota(jnp.int32, grad.shape, 1) & (cols - 1)
    for col_tap in range(3):
        shifted = grad
        if col_tap == 0:
            shifted = jnp.where(column == cols - 1, 0.0, pltpu.roll(grad, pixels - 1, 1))
        elif col_tap == 2:
            shifted = jnp.where(column == 0, 0.0, pltpu.roll(grad, 1, 1))
        for row_tap in range(3):
            tap = 3 * row_tap + col_tap
            place = slice(tap * share, (tap + 1) * share)
            if row_tap == 1:
                columns_ref[place, :] = shifted.astype(jnp.bfloat16)
                continue
            side, turn = (0, pixels - cols) if row_tap == 0 else (1, cols)
            masked = (shifted * lanes_ref[side : side + 1, :]).astype(jnp.bfloat16)
            columns_ref[place, :] = pltpu.roll(masked, turn, 1)
    part_ref[...] = jnp.dot(
        columns_ref[...], act_ref[...], preferred_element_type=jnp.float32
    ).astype(jnp.bfloat16)


def begin_back(grad_ref, weights_ref, mask_ref, taps_ref, total_ref, cols):
    clear_edges(taps_ref, cols)

    def fill(rows):
        put_taps(taps_ref, grad_ref[rows, :].astype(jnp.float32), rows, cols)

    product = product_backward(weights_ref)
    begin_conv(taps_ref, product, total_ref, fill, lambda rows, part: part, cols)
    add_rows(taps_ref, product, mask_ref, total_ref, 0, None, cols)


def finish_back(
    weights_ref, mask_ref, taps_ref, total_ref, read, table_ref, which, cols, old_ref=None
):
    mean, inverse, gain, shift = norm_rows(table_ref, which)
    scale, offset = 0.5 * inverse * gain, 0.5 * shift
    sums = []

    def slope(rows, value):
        centered = read(rows) - mean
        half = centered * scale + offset
        turn = jnp.tanh(half)
        double = value * ((1.0 + turn) * (1.0 + half * (1.0 - turn)))
        sums.append((fold(double), fold(double * centered)))
        return double

    add_rows(
        taps_ref, product_backward(weights_ref), mask_ref, total_ref, 2, slope, cols, old_ref
    )
    plain, cross = sum(pair[0] for pair in sums), sum(pair[1] for pair in sums)
    return 0.5 * plain, 0.5 * inverse * cross


def norm_back(total_ref, double, sums, read, table_ref, which, pixels, scales_ref=None):
    mean, inverse, gain, shift = norm_rows(table_ref, which)
    mean_grad, mean_cross = back_means(sums, gain, pixels)
    slope = inverse * gain * (0.5 if double else 1.0)
    level, tilt = inverse * mean_grad, inverse * inverse * mean_cross
    if scales_ref is not None:
        for row, scales in enumerate((mean, slope, level, tilt)):
            scales_ref[row : row + 1, :] = scales

    def back(rows, inner):
        return total_ref[inner, :] * slope - level - (read(rows) - mean) * tilt

    return back


def own_lanes():
    block = lax.axis_index("height") // 2
    return pl.ds(pl.multiple_of(block * NARROW, NARROW), NARROW)


def narrow_back(total_ref, value_ref, scales_ref):
    lanes = own_lanes()
    mean, slope, level, tilt = (scales_ref[row : row + 1, lanes] for row in range(4))
    return total_ref[:, lanes] * slope - level - (value_ref[:, lanes] - mean) * tilt


def turn_kernel(grad_ref, mask_ref, weights_ref, total_ref, taps_ref, *, cols):
    begin_back(grad_ref, weights_ref.at[1], mask_ref, taps_ref, total_ref, cols)


def norm_rows(table_ref, which):
    picks = (2 * which, 2 * which + 1, 6 + which, 9 + which)
    return tuple(table_ref[pick : pick + 1, :] for pick in picks)


def build_masks(ids_ref, mask_ref, lanes_ref, id_rows_ref, id_cols_ref, cols):
    rows = ids_ref.shape[1]

    def one_row(row, carry):
        here = ids_ref[0, row]
        place = pl.ds(pl.multiple_of(row * cols, cols), cols)
        id_rows_ref[place, :] = jnp.full((cols, LANES), here, jnp.int32)
        for side, other in ((0, row - 1), (1, row + 1)):
            inside = jnp.logical_and(other >= 0, other < rows)
            other_id = ids_ref[0, jnp.clip(other, 0, rows - 1)]
            same = jnp.where(jnp.logical_and(inside, other_id == here), 1.0, 0.0)
            mask_ref[side, place, :] = jnp.full((cols, LANES), same, jnp.float32)
        return carry

    lax.fori_loop(0, rows, one_row, 0)
    lane = lax.broadcasted_iota(jnp.int32, (8, LANES), 1)
    each = LANES // cols
    for block in range(rows // each):
        ids = jnp.full((8, LANES), ids_ref[0, block * each], jnp.int32)
        for step in range(1, each):
            ids = jnp.where(lane >= step * cols, ids_ref[0, block * each + step], ids)
        id_cols_ref[:, block * LANES : (block + 1) * LANES] = ids
    ids = id_cols_ref[...].astype(jnp.float32)
    pixels = ids.shape[1]
    pixel = lax.broadcasted_iota(jnp.int32, ids.shape, 1)
    above = jnp.where(pixel < cols, -1.0, pltpu.roll(ids, cols, 1))
    below = jnp.where(pixel >= pixels - cols, -1.0, pltpu.roll(ids, pixels - cols, 1))
    lanes_ref[0:1, :] = jnp.where(above == ids, 1.0, 0.0)[0:1]
    lanes_ref[1:2, :] = jnp.where(below == ids, 1.0, 0.0)[0:1]


def place_pieces(pieces, whole_ref, sems):
    own_pixels = whole_ref.shape[0] // len(pieces)
    height = lax.axis_index("height")
    copies = []
    for place, piece in enumerate(pieces):
        piece = piece.at[piece.shape[0] - own_pixels : piece.shape[0], :]
        start = pl.multiple_of((height ^ place) * own_pixels, own_pixels)
        rows = pl.ds(start, own_pixels)
        copies.append(pltpu.make_async_copy(piece, whole_ref.at[rows, :], sems.at[place]))
    return copies


def hold_kernel(
    ids_hbm,
    gains_hbm,
    shifts_hbm,
    biases_hbm,
    weights_hbm,
    qkv_hbm,
    proj_hbm,
    qv_bias_hbm,
    proj_bias_hbm,
    weights_ref,
    turned_ref,
    qkv_ref,
    proj_ref,
    table_ref,
    mask_ref,
    lanes_ref,
    id_rows_ref,
    id_cols_ref,
    ids_ref,
    gains_ref,
    shifts_ref,
    biases_ref,
    qv_bias_ref,
    proj_bias_ref,
    sems,
    *,
    cols,
):
    channels = weights_ref.shape[-1]
    small = [
        (ids_hbm, ids_ref),
        (gains_hbm, gains_ref),
        (shifts_hbm, shifts_ref),
        (biases_hbm, biases_ref),
        (qv_bias_hbm, qv_bias_ref),
        (proj_bias_hbm, proj_bias_ref),
    ]
    large = [(weights_hbm, weights_ref), (qkv_hbm, qkv_ref), (proj_hbm, proj_ref)]
    for which in range(2):
        for row_tap in range(3):
            for col_tap in range(3):
                place = slice(col_tap * channels, (col_tap + 1) * channels)
                large.append(
                    (
                        weights_hbm.at[which, 2 - row_tap, 2 - col_tap],
                        turned_ref.at[which, row_tap, :, place],
                    )
                )
    copies = [
        pltpu.make_async_copy(source, target, sems.at[index])
        for index, (source, target) in enumerate(small + large)
    ]
    for copy in copies:
        copy.start()
    for copy in copies[: len(small)]:
        copy.wait()
    build_masks(ids_ref, mask_ref, lanes_ref, id_rows_ref, id_cols_ref, cols)
    table_ref[6:9, :] = gains_ref[...]
    table_ref[9:12, :] = shifts_ref[...]
    table_ref[12:14, :] = biases_ref[...]
    table_ref[14:16, :] = qv_bias_ref[...]
    table_ref[16:17, :] = proj_bias_ref[...]
    for copy in copies[len(small) :]:
        copy.wait()


def conv_kernel(*refs, cols, count):
    pieces, refs = refs[:count], refs[count:]
    (
        weights_ref,
        params_ref,
        mask_ref,
        features_ref,
        act_one_ref,
        middle_ref,
        act_two_ref,
        residual_ref,
        table_ref,
        own_ref,
        taps_ref,
        sem,
    ) = refs
    pixels, channels = features_ref.shape
    wide = jnp.float32
    own_copy = pltpu.make_async_copy(pieces[0], own_ref, sem)
    own_copy.start()
    table_ref[...] = params_ref[...]
    clear_edges(taps_ref, cols)

    def read_input(rows):
        return features_ref[rows, :].astype(wide)

    def read_middle(rows):
        return middle_ref[rows, :]

    height = lax.axis_index("height")
    own_pixels = pixels // count
    seen = RunningStats(channels)
    for place in list(range(1, count)) + [0]:
        if place == 0:
            own_copy.wait()
        piece = (pieces[place] if place else own_ref)[0:own_pixels, :]
        start = pl.multiple_of((height ^ place) * own_pixels, own_pixels)
        features_ref[pl.ds(start, own_pixels), :] = piece
        seen.add(piece.astype(wide))
    table_ref[0:1, :], table_ref[1:2, :] = seen.finish(pixels)
    seen = RunningStats(channels)

    def keep(rows, value):
        seen.add(value)
        return value

    run_conv(
        taps_ref,
        product_forward(weights_ref.at[0]),
        mask_ref,
        middle_ref,
        activation(read_input, *norm_rows(table_ref, 0), act_one_ref, taps_ref, cols),
        lambda rows, part: part + table_ref[12:13, :],
        keep,
        cols,
    )
    table_ref[2:3, :], table_ref[3:4, :] = seen.finish(pixels)
    seen = RunningStats(channels)
    run_conv(
        taps_ref,
        product_forward(weights_ref.at[1]),
        mask_ref,
        residual_ref,
        activation(read_middle, *norm_rows(table_ref, 1), act_two_ref, taps_ref, cols),
        lambda rows, part: part + (read_input(rows) + table_ref[13:14, :]),
        keep,
        cols,
    )
    table_ref[4:5, :], table_ref[5:6, :] = seen.finish(pixels)


def score_kernel(
    qkv_ref,
    proj_ref,
    residual_ref,
    table_ref,
    id_rows_ref,
    id_cols_ref,
    normed_ref,
    query_ref,
    key_ref,
    value_ref,
    soft_ref,
    out_flip_ref,
    output_ref,
    value_flip_ref,
    *scores_refs,
    score_scale,
):
    pixels, channels = residual_ref.shape
    own_pixels = output_ref.shape[0]
    wide = jnp.float32
    exponent = score_scale * 1.4426950408889634
    mean, inverse, gain, shift = norm_rows(table_ref, 2)
    scale = inverse * gain

    def normalise(start):
        rows = slice(start, start + KEY_ROWS)
        normed = (residual_ref[rows, :] - mean) * scale + shift
        normed_ref[rows, :] = normed.astype(jnp.bfloat16)

    def project(start):
        rows = slice(start, start + KEY_ROWS)
        normed = normed_ref[rows, :]
        query_ref[rows, :] = (
            jnp.dot(normed, qkv_ref[:, 0:channels], preferred_element_type=wide)
            + table_ref[14:15, :]
        ).astype(jnp.bfloat16)
        key_ref[rows, :] = jnp.dot(
            normed, qkv_ref[:, channels : 2 * channels], preferred_element_type=wide
        ).astype(jnp.bfloat16)
        values = (
            jnp.dot(normed, qkv_ref[:, 2 * channels :], preferred_element_type=wide)
            + table_ref[15:16, :]
        ).astype(jnp.bfloat16)
        value_ref[rows, :] = values
        value_flip_ref[:, rows] = values.T

    normalise(0)
    for start in range(0, pixels, KEY_ROWS):
        if start + KEY_ROWS < pixels:
            normalise(start + KEY_ROWS)
        project(start)
    block = scores_refs[0].shape[1]
    steps = range(0, pixels, KEY_ROWS)

    def score(index):
        rows = slice(index * block, (index + 1) * block)
        for start in steps:
            keys = slice(start, start + KEY_ROWS)
            scores = lax.dot_general(
                key_ref[keys, :],
                query_ref[rows, :],
                (((1,), (1,)), ((), ())),
                preferred_element_type=wide,
            )
            same = widen(id_rows_ref[keys, :], block) == id_cols_ref[0:1, rows]
            scores_refs[index][keys, :] = jnp.where(same, scores, masked_score)

    def soften(index):
        rows = slice(index * block, (index + 1) * block)
        scores_ref = scores_refs[index]
        peak = jnp.full((8, block), masked_score, wide)
        for start in steps:
            scores = scores_ref[start : start + KEY_ROWS, :]
            peak = jnp.maximum(peak, jnp.max(scores.reshape(-1, 8, block), axis=0))
        peak = jnp.max(peak, axis=0, keepdims=True)
        total = jnp.zeros((8, block), wide)
        for start in steps:
            keys = slice(start, start + KEY_ROWS)
            powers = jnp.exp2((scores_ref[keys, :] - peak) * exponent)
            scores_ref[keys, :] = powers
            total = total + fold(powers)
        share = 1.0 / column_total(total)
        for start in steps:
            keys = slice(start, start + KEY_ROWS)
            soft_ref[keys, rows] = (scores_ref[keys, :] * share).astype(jnp.bfloat16)

    score(0)
    for index in range(len(scores_refs)):
        if index + 1 < len(scores_refs):
            score(index + 1)
        soften(index)
        rows = slice(index * block, (index + 1) * block)
        out_flip_ref[:, rows] = jnp.dot(
            value_flip_ref[...], soft_ref[:, rows], preferred_element_type=wide
        ).astype(jnp.bfloat16)
    height = lax.axis_index("height")
    own = pl.ds(pl.multiple_of(height * own_pixels, own_pixels), own_pixels)
    output_ref[...] = (
        residual_ref[own, :]
        + lax.dot_general(
            out_flip_ref[:, own],
            proj_ref[...],
            (((0,), (0,)), ((), ())),
            preferred_element_type=wide,
        )
        + table_ref[16:17, :]
    ).astype(jnp.bfloat16)


def own_quarter():
    height = lax.axis_index("height")
    return (height & 1) * 2 + ((height >> 1) & 1)


def attention_kernel(
    proj_ref,
    normed_ref,
    query_ref,
    key_ref,
    value_ref,
    soft_ref,
    out_flip_ref,
    *refs,
    score_scale,
    count,
):
    pieces, (grad_ref, packed_ref, sums_ref), refs = (
        refs[:count],
        refs[count : count + 3],
        refs[count + 3 :],
    )
    pixels, channels = normed_ref.shape
    blocks = pixels // SCORE_ROWS
    grads_refs, refs = refs[-blocks:], refs[:-blocks]
    keep_ref, send_ref, mixed_ref, key_flip_ref, back_ref, score_grad_ref, flip_ref, sems = refs
    wide = jnp.float32
    copies = place_pieces(pieces, grad_ref, sems)
    for copy in copies:
        copy.start()
    quarter = channels // 4
    own = pl.ds(pl.multiple_of(own_quarter() * quarter, quarter), quarter)
    flip_ref[...] = normed_ref[:, own].T
    key_flip_ref[...] = key_ref[...].T
    for copy in copies:
        copy.wait()
    block, count = SCORE_ROWS, blocks
    steps = range(0, pixels, KEY_ROWS)

    def block_rows(index):
        return slice(index * block, (index + 1) * block)

    for index in range(count):
        back_ref[block_rows(index), :] = lax.dot_general(
            grad_ref[block_rows(index), :],
            proj_ref[...],
            (((1,), (1,)), ((), ())),
            preferred_element_type=wide,
        ).astype(jnp.bfloat16)

    def weigh(index):
        total = jnp.zeros((8, block), wide)
        for start in steps:
            keys = slice(start, start + KEY_ROWS)
            weight_grad = lax.dot_general(
                value_ref[keys, :],
                back_ref[block_rows(index), :],
                (((1,), (1,)), ((), ())),
                preferred_element_type=wide,
            )
            grads_refs[index][keys, :] = weight_grad
            total = total + fold(soft_ref[keys, block_rows(index)].astype(wide) * weight_grad)
        return column_total(total)

    def slope(index, dots):
        for start in steps:
            keys = slice(start, start + KEY_ROWS)
            weights = soft_ref[keys, block_rows(index)].astype(wide)
            score_grad_ref[keys, block_rows(index)] = (
                weights * (grads_refs[index][keys, :] - dots)
            ).astype(jnp.bfloat16)

    dots = weigh(0)
    for index in range(count):
        now, rows = dots, block_rows(index)
        if index + 1 < count:
            dots = weigh(index + 1)
        slope(index, now)
        packed_ref[rows, 2 * channels :] = jnp.dot(
            soft_ref[rows, :], back_ref[...], preferred_element_type=wide
        ).astype(jnp.bfloat16)
        query_grad = jnp.dot(
            key_flip_ref[...], score_grad_ref[:, rows], preferred_element_type=wide
        )
        packed_ref[rows, 0:channels] = (query_grad * score_scale).astype(jnp.bfloat16).T
    for index in range(count):
        rows = block_rows(index)
        packed_ref[rows, channels : 2 * channels] = (
            jnp.dot(score_grad_ref[rows, :], query_ref[...], preferred_element_type=wide)
            * score_scale
        ).astype(jnp.bfloat16)

    def pack(rows, carry):
        return (
            carry[0] + fold(packed_ref[rows, 0:channels].astype(wide)),
            carry[1] + fold(packed_ref[rows, 2 * channels :].astype(wide)),
            carry[2] + fold(grad_ref[rows, :].astype(wide)),
        )

    zeros = jnp.zeros((8, channels), wide)
    totals = zeros, zeros, zeros
    for start in range(0, pixels, CHUNK):
        totals = pack(pl.ds(start, CHUNK), totals)
    sums_ref[...] = jnp.zeros(sums_ref.shape, wide)
    for row, total in enumerate(totals):
        sums_ref[8 + row : 9 + row, :] = column_total(total)
    mixed_ref[:, 0 : 3 * channels] = jnp.dot(
        flip_ref[...], packed_ref[...], preferred_element_type=wide
    ).astype(jnp.bfloat16)
    mixed_ref[:, 3 * channels :] = jnp.dot(
        out_flip_ref[own, :], grad_ref[...], preferred_element_type=wide
    ).astype(jnp.bfloat16)
    keep_half(mixed_ref, 0, keep_ref, send_ref)


def third_kernel(
    qkv_ref,
    grad_ref,
    packed_ref,
    residual_ref,
    table_ref,
    act_two_ref,
    lanes_ref,
    old_sums_ref,
    residual_grad_ref,
    grad_two_ref,
    sums_ref,
    part_ref,
    total_ref,
    flip_ref,
    columns_ref,
    *,
    cols,
):
    pixels, channels = residual_ref.shape
    block = FILL_ROWS
    wide = jnp.float32
    mean, inverse, gain, shift = norm_rows(table_ref, 2)
    zeros = jnp.zeros((8, channels), wide)

    sums = (zeros, zeros)
    for start in range(0, pixels, block):
        rows = pl.ds(start, block)
        normed_grad = lax.dot_general(
            packed_ref[rows, :], qkv_ref[...], (((1,), (1,)), ((), ())), preferred_element_type=wide
        )
        total_ref[rows, :] = normed_grad
        centered = residual_ref[rows, :] - mean
        sums = sums[0] + fold(normed_grad), sums[1] + fold(normed_grad * centered)
    sums = sums[0], sums[1] * inverse
    sums_ref[...] = old_sums_ref[...]
    sums_ref[5:6, :] = column_total(sums[1])
    sums_ref[6:7, :] = column_total(sums[0])
    back = norm_back(
        total_ref, False, sums, lambda rows: residual_ref[rows, :], table_ref, 2, pixels
    )

    def finish(rows, carry):
        total = grad_ref[rows, :].astype(wide) + back(rows, rows)
        residual_grad_ref[rows, :] = total
        low = total.astype(jnp.bfloat16)
        grad_two_ref[rows, :] = low
        return carry + fold(low.astype(wide))

    sums_ref[7:8, :] = column_total(each_chunk(pixels, finish, zeros))
    narrow = grad_two_ref[:, own_lanes()]
    weight_part(act_two_ref, narrow, lanes_ref, flip_ref, columns_ref, part_ref, cols)


def second_kernel(
    old_total_ref,
    taps_ref,
    middle_ref,
    table_ref,
    act_one_ref,
    mask_ref,
    lanes_ref,
    weights_ref,
    old_sums_ref,
    part_two_ref,
    grad_one_ref,
    sums_ref,
    keep_one_ref,
    send_one_ref,
    keep_two_ref,
    send_two_ref,
    total_ref,
    flip_ref,
    columns_ref,
    part_ref,
    scales_ref,
    *,
    cols,
):
    pixels, channels = middle_ref.shape

    def read(rows):
        return middle_ref[rows, :]

    sums = finish_back(
        weights_ref.at[1], mask_ref, taps_ref, total_ref, read, table_ref, 1, cols, old_total_ref
    )
    back = norm_back(total_ref, True, sums, read, table_ref, 1, pixels, scales_ref)
    narrow = narrow_back(total_ref, middle_ref, scales_ref).astype(jnp.bfloat16)
    weight_part(act_one_ref, narrow, lanes_ref, flip_ref, columns_ref, part_ref, cols)
    sums_ref[...] = old_sums_ref[...]
    sums_ref[2:3, :] = column_total(sums[1])
    sums_ref[3:4, :] = column_total(sums[0])

    def finish(rows, carry):
        low = back(rows, rows).astype(jnp.bfloat16)
        grad_one_ref[rows, :] = low
        return carry + fold(low.astype(jnp.float32))

    zeros = jnp.zeros((8, channels), jnp.float32)
    sums_ref[4:5, :] = column_total(each_chunk(pixels, finish, zeros))
    keep_half(part_ref, 1, keep_one_ref, send_one_ref)
    keep_half(part_two_ref, 1, keep_two_ref, send_two_ref)


def near_far():
    core = lax.axis_index("height") & 1
    return 1 + core, 2 - core


def keep_half(source_ref, axis, keep_ref, send_ref):
    me = lax.axis_index("canvas")
    near, far = near_far()
    rows, width = keep_ref.shape[0] // 2, keep_ref.shape[1]
    for target_ref, flip in ((keep_ref, 0), (send_ref, near)):
        for slot, other in enumerate((0, far)):
            owner = me ^ flip ^ other
            target = target_ref.at[slot * rows : (slot + 1) * rows, :]
            if axis == 0:
                target[...] = source_ref[pl.ds(pl.multiple_of(owner * rows, rows), rows), :]
            else:
                target[...] = source_ref[:, pl.ds(pl.multiple_of(owner * width, width), width)]


def first_kernel(
    grad_one_ref,
    features_ref,
    table_ref,
    mask_ref,
    old_sums_ref,
    weights_ref,
    own_ref,
    sums_ref,
    partial_ref,
    total_ref,
    taps_ref,
    *,
    cols,
):
    def read(rows):
        return features_ref[rows, :].astype(jnp.float32)

    weights = weights_ref.at[0]
    begin_back(grad_one_ref, weights, mask_ref, taps_ref, total_ref, cols)
    sums = finish_back(weights, mask_ref, taps_ref, total_ref, read, table_ref, 0, cols)
    partial_ref[0:8, :], partial_ref[8:16, :] = sums
    sums_ref[...] = old_sums_ref[...]
    sums_ref[0:1, :] = column_total(sums[1])
    sums_ref[1:2, :] = column_total(sums[0])
    count = own_ref.shape[0]
    own = pl.ds(pl.multiple_of(lax.axis_index("height") * count, count), count)
    own_ref[...] = total_ref[own, :]


def own_kernel(
    own_ref, partial_ref, features_ref, residual_grad_ref, table_ref, input_grad_ref
):
    def read(rows):
        return features_ref[rows, :].astype(jnp.float32)

    sums = partial_ref[0:8, :], partial_ref[8:16, :]
    pixels = features_ref.shape[0]
    back = norm_back(own_ref, True, sums, read, table_ref, 0, pixels)
    count = own_ref.shape[0]
    own = pl.ds(pl.multiple_of(lax.axis_index("height") * count, count), count)
    total = residual_grad_ref[own, :] + back(own, slice(0, count))
    input_grad_ref[...] = total.astype(jnp.bfloat16)


def place_kernel(*refs):
    joints, packed_ref = refs[:-1], refs[-1]
    share = packed_ref.shape[0] // len(joints)
    me = lax.axis_index("canvas")
    for step, joint in enumerate(joints):
        place = pl.ds(pl.multiple_of((me ^ step) * share, share), share)
        packed_ref[place, :] = joint[...]


def cut_kernel(packed_ref, *half_refs):
    rows = half_refs[0].shape[0]
    for index, half_ref in enumerate(half_refs):
        half_ref[...] = packed_ref[index * rows : (index + 1) * rows, :]


def spread_quarters(packed, flips, qkv_ref, proj_ref, qkv_hbm, proj_hbm, sems):
    quarter = packed[0].shape[0]
    inner = qkv_ref.shape[2]
    copies = []
    for index, packed_ref in enumerate(packed):
        owner = own_quarter() ^ flips[index]
        rows = pl.ds(pl.multiple_of(owner * quarter, quarter), quarter)
        qkv_ref[index] = packed_ref[:, 0:inner].astype(jnp.float32)
        proj_ref[index] = packed_ref[:, inner:].astype(jnp.float32)
        for which, (held, target) in enumerate(((qkv_ref, qkv_hbm), (proj_ref, proj_hbm))):
            copy = pltpu.make_async_copy(held.at[index], target.at[rows, :], sems.at[index, which])
            copy.start()
            copies.append(copy)
    return copies


def join_kernel(*refs):
    packed, (qkv_hbm, proj_hbm, qkv_ref, proj_ref, sems) = refs[:-5], refs[-5:]
    copies = spread_quarters(packed, [0, 2], qkv_ref, proj_ref, qkv_hbm, proj_hbm, sems)
    for copy in copies:
        copy.wait()


def halve_kernel(keep_ref, got_ref, hold_ref, send_ref):
    total = keep_ref[...].astype(jnp.float32) + got_ref[...].astype(jnp.float32)
    rows = hold_ref.shape[0]
    hold_ref[...] = total[0:rows]
    send_ref[0:rows, :] = total[rows:].astype(jnp.bfloat16)


def halve_both_kernel(
    keep_ref, got_ref, keep_two_ref, got_two_ref, hold_ref, send_ref, hold_two_ref
):
    rows = hold_ref.shape[0]
    halve_kernel(keep_ref, got_ref, hold_ref, send_ref)
    halve_kernel(keep_two_ref, got_two_ref, hold_two_ref, send_ref.at[rows : 2 * rows, :])


def last_kernel(
    chip_ref,
    both_a_ref,
    both_b_ref,
    old_qkv,
    old_proj,
    qkv_hbm,
    proj_hbm,
    qkv_ref,
    proj_ref,
    sems,
):
    copies = []
    rows = both_a_ref.shape[0]
    inner = qkv_ref.shape[2]
    chips = (chip_ref.at[0:rows, :], chip_ref.at[rows : 2 * rows, :])
    for index, piece_ref in enumerate((*chips, both_a_ref, both_b_ref)):
        start = ((own_quarter() ^ (1 if index < 2 else 3)) * 2 + index % 2) * rows
        target = pl.ds(pl.multiple_of(start, rows), rows)
        qkv_ref[index] = piece_ref[:, 0:inner].astype(jnp.float32)
        proj_ref[index] = piece_ref[:, inner:].astype(jnp.float32)
        for which, (held, whole) in enumerate(((qkv_ref, qkv_hbm), (proj_ref, proj_hbm))):
            copy = pltpu.make_async_copy(held.at[index], whole.at[target, :], sems.at[index, which])
            copy.start()
            copies.append(copy)
    for copy in copies:
        copy.wait()


def sums_kernel(
    sums_ref,
    got_sums_ref,
    hold_one_ref,
    hold_two_ref,
    got_ref,
    share_ref,
    gains_ref,
    shifts_ref,
    conv_ref,
    qv_ref,
    bias_ref,
):
    rows = hold_one_ref.shape[0]
    for which, hold_ref in enumerate((hold_one_ref, hold_two_ref)):
        got = got_ref[which * rows : (which + 1) * rows, :].astype(jnp.float32)
        share_ref[which] = (hold_ref[...] + got).reshape(share_ref.shape[1:])
    total = sums_ref[...] + got_sums_ref[...]
    for row, start in enumerate((0, 2, 5)):
        gains_ref[row : row + 1, :] = total[start : start + 1]
        shifts_ref[row : row + 1, :] = total[start + 1 : start + 2]
    conv_ref[0:1, :] = total[4:5]
    conv_ref[1:2, :] = total[7:8]
    qv_ref[...] = total[8:10]
    bias_ref[...] = total[10:11]


def call_kernel(kernel, outputs, scratch, operands, places, flops, limit, out_places=None, aliases={}):
    out_places = out_places or "v" * len(outputs)
    spaces = {
        "v": pl.BlockSpec(memory_space=pltpu.VMEM),
        "s": pl.BlockSpec(memory_space=pltpu.SMEM),
        "h": pl.BlockSpec(memory_space=pl.ANY),
        "o": pl.BlockSpec(memory_space=pltpu.VMEM),
        "a": pl.BlockSpec(memory_space=pl.ANY),
    }
    moved = 8 * flops // LANES
    held = {"v": pltpu.VMEM, "h": pltpu.HBM, "o": jax.ShapeDtypeStruct}
    operands = [
        pltpu.with_memory_space_constraint(array, pltpu.HBM) if place == "h" else array
        for array, place in zip(operands, places)
    ]
    return pl.pallas_call(
        kernel,
        out_shape=[held[place](*output) for output, place in zip(outputs, out_places)],
        in_specs=[spaces[place] for place in places],
        out_specs=[spaces[place] for place in out_places],
        scratch_shapes=scratch,
        input_output_aliases=aliases,
        compiler_params=pltpu.CompilerParams(vmem_limit_bytes=limit * 2**20),
        cost_estimate=pl.CostEstimate(flops=flops, bytes_accessed=moved, transcendentals=0),
    )(*operands)


def send_height(block, step):
    size = lax.axis_size("height")
    return lax.ppermute(block, "height", [(i, i ^ step) for i in range(size)])


def with_cores(blocks, other):
    pieces = [blocks[0], other]
    for block in blocks[1:]:
        pieces += [block, send_height(block, 1)]
    return pieces


def send_canvas(block, step):
    size = lax.axis_size("canvas")
    return lax.ppermute(block, "canvas", [(i, i ^ step) for i in range(size)])


def send_phase(block, phase):
    canvases, size = lax.axis_size("canvas"), lax.axis_size("height")
    pairs = []
    for canvas in range(canvases):
        for height in range(size):
            step = 2 if (height ^ phase) & 1 else 1
            pairs.append((canvas * size + height, (canvas ^ step) * size + height))
    return lax.ppermute(block, ("canvas", "height"), pairs)


def trade_canvas(pieces):
    return [pieces[0]] + [send_canvas(piece, step) for step, piece in enumerate(pieces) if step]


def whole_canvas(
    features,
    tile_ids,
    norm_gains,
    norm_shifts,
    conv_weights,
    conv_biases,
    qkv_weight,
    qv_bias,
    proj_weight,
    proj_bias,
    cotangent,
):
    height_size = lax.axis_size("height")
    canvas_size = lax.axis_size("canvas")
    local_rows, cols, channels = features.shape[1:]
    all_rows = tile_ids.shape[1]
    pixels = all_rows * cols
    own_pixels = local_rows * cols
    out_share = channels // height_size
    ci_share = channels // canvas_size
    quarter = channels // 4
    row_share = quarter // canvas_size
    low, wide = jnp.bfloat16, jnp.float32

    own_features = features.reshape(own_pixels, channels)
    own_grad = cotangent.reshape(own_pixels, channels)
    steps = range(2, height_size, 2)
    held_features = [own_features] + [send_height(own_features, step) for step in steps]
    plane = ((pixels, channels), low)
    plane_wide = ((pixels, channels), wide)
    sums_shape = ((16, channels), wide)
    mixed_halves = [((2 * row_share, 4 * channels), low)] * 2
    taps = pltpu.VMEM((pixels + 2 * cols, 3 * channels), low)
    held_wide = pltpu.VMEM((pixels, channels), wide)
    flipped = pltpu.VMEM((channels, pixels), low)
    narrow = pltpu.VMEM((NARROW, pixels), low)
    columns = pltpu.VMEM((9 * out_share, pixels), low)
    part_held = pltpu.VMEM((9 * out_share, channels), low)
    sem = pltpu.SemaphoreType.DMA
    conv_flops = 2 * 9 * pixels * channels * channels
    dot_flops = 2 * pixels * channels * channels
    score_flops = 2 * pixels * pixels * channels
    scale = channels ** (-0.5)

    (
        held_conv,
        turned,
        held_qkv,
        held_proj,
        params,
        mask,
        lane_mask,
        id_rows,
        id_cols,
    ) = call_kernel(
        functools.partial(hold_kernel, cols=cols),
        [
            (conv_weights.shape, low),
            ((2, 3, channels, 3 * channels), low),
            (qkv_weight.shape, low),
            (proj_weight.shape, low),
            ((24, channels), wide),
            ((2, pixels, LANES), wide),
            ((8, pixels), wide),
            ((pixels, LANES), jnp.int32),
            ((8, pixels), jnp.int32),
        ],
        [
            pltpu.SMEM(tile_ids.shape, jnp.int32),
            pltpu.VMEM(norm_gains.shape, wide),
            pltpu.VMEM(norm_shifts.shape, wide),
            pltpu.VMEM(conv_biases.shape, wide),
            pltpu.VMEM(qv_bias.shape, wide),
            pltpu.VMEM((1, channels), wide),
            sem((27,)),
        ],
        [
            tile_ids,
            norm_gains,
            norm_shifts,
            conv_biases,
            conv_weights,
            qkv_weight,
            proj_weight,
            qv_bias,
            proj_bias.reshape(1, channels),
        ],
        "h" * 9,
        conv_flops,
        8,
    )
    held_features[1:] = [
        lax.optimization_barrier((params, block))[1] for block in held_features[1:]
    ]
    other_core = send_height(jnp.concatenate([own_features, own_grad], axis=0), 1)
    pieces = with_cores(held_features, other_core)
    far_grad, *pieces[4::2] = lax.optimization_barrier((own_grad, *held_features[2:]))
    held_grads = [own_grad, send_height(own_grad, 2)]
    held_grads[1], pieces[2] = lax.optimization_barrier((held_grads[1], held_features[1]))
    held_grads += [send_height(far_grad, step) for step in steps[1:]]

    all_features, act_one, middle, act_two, residual, table = call_kernel(
        functools.partial(conv_kernel, cols=cols, count=height_size),
        [plane, plane, plane_wide, plane, plane_wide, ((24, channels), wide)],
        [pltpu.VMEM((own_pixels, channels), low), taps, sem],
        [*pieces, held_conv, params, mask],
        "h" + "v" * (height_size + 2),
        2 * conv_flops,
        16,
    )
    residual, *held_grads = lax.optimization_barrier((residual, *held_grads))
    grad_pieces = with_cores(held_grads, other_core)
    normed, query, key, value, soft, out_flip, output = call_kernel(
        functools.partial(score_kernel, score_scale=scale),
        [
            plane,
            plane,
            plane,
            plane,
            ((pixels, pixels), low),
            ((channels, pixels), low),
            ((own_pixels, channels), low),
        ],
        [
            flipped,
            *[pltpu.VMEM((pixels, SCORE_ROWS), wide)] * (pixels // SCORE_ROWS),
        ],
        [
            held_qkv,
            held_proj,
            residual,
            table,
            id_rows,
            id_cols,
        ],
        "vvvvvv",
        3 * dot_flops + 2 * score_flops,
        20,
        "v" * 6 + "o",
    )
    normed, *grad_pieces = lax.optimization_barrier((normed, *grad_pieces))
    all_grad, packed, sums, keep_mixed, send_mixed = call_kernel(
        functools.partial(attention_kernel, score_scale=scale, count=height_size),
        [plane, ((pixels, 3 * channels), low), sums_shape, *mixed_halves],
        [
            pltpu.VMEM((quarter, 4 * channels), low),
            flipped,
            pltpu.VMEM((pixels, channels), low),
            pltpu.VMEM((pixels, pixels), low),
            pltpu.VMEM((quarter, pixels), low),
            sem((height_size,)),
            *[pltpu.VMEM((pixels, SCORE_ROWS), wide)] * (pixels // SCORE_ROWS),
        ],
        [held_proj, normed, query, key, value, soft, out_flip, *grad_pieces],
        "vvvvvvvh" + "a" * (height_size - 1),
        3 * dot_flops + 4 * score_flops,
        20,
    )
    got_mixed = send_phase(send_mixed, 0)
    residual_grad, grad_two, sums, part_two = call_kernel(
        functools.partial(third_kernel, cols=cols),
        [plane_wide, plane, sums_shape, ((9 * out_share, channels), low)],
        [held_wide, narrow, columns],
        [held_qkv, all_grad, packed, residual, table, act_two, lane_mask, sums],
        "vvvvvvvv",
        3 * dot_flops + conv_flops // height_size,
        16,
    )
    grad_two, got_mixed = lax.optimization_barrier((grad_two, got_mixed))
    hold_mixed, send_mixed = call_kernel(
        halve_kernel,
        [((row_share, 4 * channels), kind) for kind in (wide, low)],
        [],
        [keep_mixed, got_mixed],
        "vv",
        1,
        12,
    )
    got_mixed = send_phase(send_mixed, 1)
    grad_two, hold_mixed = lax.optimization_barrier((grad_two, hold_mixed))
    half_total, half_taps = call_kernel(
        functools.partial(turn_kernel, cols=cols),
        [plane_wide, (taps.shape, low)],
        [],
        [grad_two, mask, turned],
        "vvv",
        2 * conv_flops // 3,
        16,
    )
    half_total, got_mixed = lax.optimization_barrier((half_total, got_mixed))
    mixed_sum = (hold_mixed + got_mixed.astype(wide)).astype(low)
    joints = trade_canvas([mixed_sum] * canvas_size)
    halves = [((2 * 9 * out_share, ci_share), low)] * 4
    grad_one, sums, keep_one, send_one, keep_two, send_two = call_kernel(
        functools.partial(second_kernel, cols=cols),
        [plane, sums_shape, *halves],
        [held_wide, narrow, columns, part_held, pltpu.VMEM((8, channels), wide)],
        [half_total, half_taps, middle, table, act_one, mask, lane_mask, turned, sums, part_two],
        "v" * 10,
        conv_flops // 2,
        20,
    )
    grad_one, *joints = lax.optimization_barrier((grad_one, *joints))
    (own_mixed,) = call_kernel(
        place_kernel,
        [((quarter, 4 * channels), low)],
        [],
        joints,
        "v" * canvas_size,
        1,
        12,
    )
    own_mixed, send_one, send_two = lax.optimization_barrier((own_mixed, send_one, send_two))
    chip_mixed = send_height(own_mixed, 2)
    core_mixed = send_height(own_mixed, 1)
    got_one, got_two = send_phase(send_one, 0), send_phase(send_two, 0)
    own_total, sums, partial_sums = call_kernel(
        functools.partial(first_kernel, cols=cols),
        [((own_pixels, channels), wide), sums_shape, sums_shape],
        [held_wide, taps],
        [grad_one, all_features, table, mask, sums, turned],
        "vvvvvv",
        1,
        20,
    )
    got_sums, own_sums = send_phase(sums, 0), sums
    sums, core_mixed, got_one, got_two = lax.optimization_barrier(
        (sums, core_mixed, got_one, got_two)
    )
    share_rows = 9 * out_share
    hold_one, send_share, hold_two = call_kernel(
        halve_both_kernel,
        [
            ((share_rows, ci_share), wide),
            ((2 * share_rows, ci_share), low),
            ((share_rows, ci_share), wide),
        ],
        [],
        [keep_one, got_one, keep_two, got_two],
        "vvvv",
        1,
        12,
    )
    got_share = send_phase(send_share, 1)

    def widened(count, rows):
        return [
            pltpu.VMEM((count, rows, 3 * channels), wide),
            pltpu.VMEM((count, rows, channels), wide),
            sem((count, 2)),
        ]

    grad_shapes = [(qkv_weight.shape, wide), (proj_weight.shape, wide)]
    core_mixed, hold_one = lax.optimization_barrier((core_mixed, hold_one))
    qkv_grad, proj_grad = call_kernel(
        join_kernel,
        grad_shapes,
        widened(2, quarter),
        [own_mixed, core_mixed],
        "vv",
        1,
        12,
        "hh",
    )
    qkv_grad, chip_mixed, got_sums = lax.optimization_barrier((qkv_grad, chip_mixed, got_sums))
    sums = own_sums + got_sums
    got_sums = send_phase(sums, 1)
    chip_halves = call_kernel(
        cut_kernel,
        [((quarter // 2, 4 * channels), low)] * 2,
        [],
        [chip_mixed],
        "v",
        1,
        12,
    )
    both_halves = [send_height(half, 1) for half in chip_halves]
    qkv_grad, proj_grad = call_kernel(
        last_kernel,
        grad_shapes,
        widened(4, quarter // 2),
        [chip_mixed, *both_halves, qkv_grad, proj_grad],
        "vvvhh",
        1,
        12,
        "hh",
        {3: 0, 4: 1},
    )
    qkv_grad, own_total = lax.optimization_barrier((qkv_grad, own_total))
    (input_grad,) = call_kernel(
        own_kernel,
        [((own_pixels, channels), low)],
        [],
        [own_total, partial_sums, all_features, residual_grad, table],
        "vvvvv",
        dot_flops // 4,
        12,
        "o",
    )
    input_grad, got_share, got_sums = lax.optimization_barrier((input_grad, got_share, got_sums))
    vector_shapes = [norm_gains.shape, norm_shifts.shape, conv_biases.shape, qv_bias.shape]
    conv_grad, gains_grad, shifts_grad, biases_grad, qv_grad, proj_bias_grad = call_kernel(
        sums_kernel,
        [((2, 3, 3, out_share, ci_share), wide)]
        + [(shape, wide) for shape in vector_shapes + [(1, channels)]],
        [],
        [sums, got_sums, hold_one, hold_two, got_share],
        "vvvvv",
        1,
        12,
        "o" * 6,
    )
    own_shape = (1, local_rows, cols, channels)
    return (
        output.reshape(own_shape),
        input_grad.reshape(own_shape),
        gains_grad,
        shifts_grad,
        jnp.swapaxes(conv_grad, 3, 4),
        biases_grad,
        qkv_grad,
        qv_grad,
        proj_grad,
        proj_bias_grad.reshape(channels),
    )


def on_device(*arrays):
    features, tile_ids = arrays[0], arrays[1]
    local_rows, cols, channels = features.shape[1:]
    pixels = tile_ids.shape[1] * cols
    height_size, canvas_size = lax.axis_size("height"), lax.axis_size("canvas")
    powers = all(size & (size - 1) == 0 for size in (height_size, canvas_size, cols))
    fits = (
        powers
        and height_size > 2
        and canvas_size == 4
        and channels == LANES * canvas_size
        and pixels <= MOST_PIXELS
        and pixels % FILL_ROWS == 0
        and FILL_ROWS % CHUNK == 0
        and pixels % SCORE_ROWS == 0
        and pixels % KEY_ROWS == 0
        and (local_rows * cols) % LANES == 0
        and CHUNK % cols == 0
        and cols % 16 == 0
        and channels % (LANES * canvas_size) == 0
        and 2 * channels == NARROW * height_size
    )
    return whole_canvas(*arrays) if fits else split_canvas(*arrays)


def solution(mesh):
    in_specs = (
        P("canvas", "height", None, None),
        P("canvas", None),
        P(),
        P(),
        P(),
        P(),
        P(),
        P(),
        P(),
        P(),
        P("canvas", "height", None, None),
    )
    out_specs = (
        P("canvas", "height", None, None),
        P("canvas", "height", None, None),
        P(),
        P(),
        P(None, None, None, "canvas", "height"),
        P(),
        P(),
        P(),
        P(),
        P(),
    )
    return jax.shard_map(
        on_device, mesh=mesh, in_specs=in_specs, out_specs=out_specs, check_vma=False
    )
```

```python
import functools

import jax
import jax.numpy as jnp
from jax import lax
from jax.experimental import pallas as pl
from jax.experimental.pallas import tpu as pltpu
from jax.sharding import PartitionSpec as P

GROUPS = 32


epsilon = 1e-06
masked_score = -1e30
MOST_PIXELS = 1024
LANES = 128
NARROW = 128
CHUNK = 128
FILL_ROWS = 256
EARLY_ROWS = 512
SCORE_ROWS = 256
KEY_ROWS = 256


def extended(block, sides, width):
    for axis, dim in sides:
        count = lax.axis_size(axis)
        forward = [(i, i + 1) for i in range(count - 1)]
        backward = [(target, source) for source, target in forward]
        low = lax.ppermute(
            lax.slice_in_dim(block, block.shape[dim] - width, None, axis=dim), axis, forward
        )
        high = lax.ppermute(lax.slice_in_dim(block, 0, width, axis=dim), axis, backward)
        block = jnp.concatenate([low, block, high], axis=dim)
    return block


def group_total(vector):
    return vector.reshape(GROUPS, -1).sum(axis=1)


def spread_groups(vector, channels):
    return jnp.repeat(vector, channels // GROUPS)


def norm_forward(values, gain, shift, members):
    channels = values.shape[1]
    totals = lax.psum(group_total(jnp.sum(values, axis=0)), "height")
    centered = values - spread_groups(totals / members, channels)
    squares = lax.psum(group_total(jnp.sum(centered * centered, axis=0)), "height")
    inverse = spread_groups(lax.rsqrt(squares / members + epsilon), channels)
    normed = centered * inverse
    return (normed, inverse, normed * gain + shift)


def norm_backward(grad_in, normed, inverse, gain, members):
    channels = grad_in.shape[1]
    scaled = grad_in * gain
    both_sums = lax.psum(
        (group_total(jnp.sum(scaled, axis=0)), group_total(jnp.sum(scaled * normed, axis=0))),
        "height",
    )
    mean_grad = spread_groups(both_sums[0] / members, channels)
    mean_cross = spread_groups(both_sums[1] / members, channels)
    result = inverse * (scaled - mean_grad - normed * mean_cross)
    return (result, jnp.sum(grad_in * normed, axis=0), jnp.sum(grad_in, axis=0))


def swish(values):
    return values * jax.nn.sigmoid(values)


def swish_slope(values):
    sigmoid_part = jax.nn.sigmoid(values)
    return sigmoid_part * (1.0 + values * (1.0 - sigmoid_part))


def tap_columns(padded, row_mask, local_rows, canvas_cols):
    pieces = []
    for row_tap in range(3):
        rows_taken = padded[row_tap : row_tap + local_rows] * row_mask[:, row_tap, None, None]
        for col_tap in range(3):
            pieces.append(rows_taken[:, col_tap : col_tap + canvas_cols])
    stacked = jnp.concatenate(pieces, axis=2)
    return stacked.reshape(local_rows * canvas_cols, stacked.shape[2])


def conv_forward(acts, row_mask, weight, bias):
    local_rows, canvas_cols, channels = acts.shape
    rimmed = extended(acts, (("height", 0),), 1)
    padded = jnp.pad(rimmed, ((0, 0), (1, 1), (0, 0)))
    gathered = tap_columns(padded, row_mask, local_rows, canvas_cols)
    result = (
        jnp.dot(
            gathered, weight.reshape(9 * channels, channels), preferred_element_type=jnp.float32
        )
        + bias
    )
    return (result, gathered)


def conv_backward(grad_low, row_mask, weight, gathered):
    local_rows, canvas_cols, channels = grad_low.shape
    flat_grad = grad_low.reshape(local_rows * canvas_cols, channels)
    weight_grad = lax.dot_general(
        gathered, flat_grad, (((0,), (0,)), ((), ())), preferred_element_type=jnp.float32
    )
    rimmed = extended(grad_low, (("height", 0),), 1)
    padded = jnp.pad(rimmed, ((0, 0), (1, 1), (0, 0)))
    grad_taps = tap_columns(padded, row_mask, local_rows, canvas_cols)
    flipped = jnp.transpose(weight[::-1, ::-1], (0, 1, 3, 2)).reshape(9 * channels, channels)
    input_part = jnp.dot(grad_taps, flipped, preferred_element_type=jnp.float32)
    return (
        input_part,
        weight_grad.reshape(3, 3, channels, channels),
        jnp.sum(flat_grad.astype(jnp.float32), axis=0),
    )


def take_rows(array, offset, count):
    return lax.dynamic_slice_in_dim(array, offset, count)


def score_grads(
    queries, out_grad, log_total, row_dots, query_ids, key_rows, value_rows, key_ids, score_scale
):
    scores = (
        lax.dot_general(
            queries, key_rows, (((1,), (1,)), ((), ())), preferred_element_type=jnp.float32
        )
        * score_scale
    )
    same_tile = query_ids[:, None] == key_ids[None, :]
    softmax_block = jnp.exp(jnp.where(same_tile, scores - log_total[:, None], masked_score))
    weight_grad = lax.dot_general(
        out_grad, value_rows, (((1,), (1,)), ((), ())), preferred_element_type=jnp.float32
    )
    score_grad = (softmax_block * (weight_grad - row_dots[:, None])).astype(jnp.bfloat16)
    return (softmax_block.astype(jnp.bfloat16), score_grad)


def split_canvas(
    features,
    tile_ids,
    norm_gains,
    norm_shifts,
    conv_weights,
    conv_biases,
    qkv_weight,
    qv_bias,
    proj_weight,
    proj_bias,
    cotangent,
):
    height_size = lax.axis_size("height")
    local_rows = features.shape[1]
    canvas_cols = features.shape[2]
    channels = features.shape[3]
    pixels = local_rows * canvas_cols
    row_ids = tile_ids[0]
    all_rows = row_ids.shape[0]
    members = float(all_rows * canvas_cols * (channels // GROUPS))
    score_scale = channels ** (-0.5)
    first_row = lax.axis_index("height") * local_rows
    edge_ids = jnp.full((1,), -1, jnp.int32)
    padded_ids = jnp.concatenate([edge_ids, row_ids, edge_ids])
    near_ids = lax.dynamic_slice_in_dim(padded_ids, first_row, local_rows + 2)
    own_rows = near_ids[1 : local_rows + 1]
    row_mask = jnp.stack(
        [near_ids[row_tap : row_tap + local_rows] == own_rows for row_tap in range(3)], axis=1
    ).astype(jnp.bfloat16)
    key_ids = jnp.repeat(row_ids, canvas_cols)
    query_ids = jnp.repeat(own_rows, canvas_cols)
    grid_shape = (local_rows, canvas_cols, channels)
    inputs = features[0].reshape(pixels, channels).astype(jnp.float32)
    normed_one, inverse_one, pre_one = norm_forward(inputs, norm_gains[0], norm_shifts[0], members)
    act_one = swish(pre_one).astype(jnp.bfloat16).reshape(grid_shape)
    middle, taps_one = conv_forward(act_one, row_mask, conv_weights[0], conv_biases[0])
    normed_two, inverse_two, pre_two = norm_forward(middle, norm_gains[1], norm_shifts[1], members)
    act_two = swish(pre_two).astype(jnp.bfloat16).reshape(grid_shape)
    branch, taps_two = conv_forward(act_two, row_mask, conv_weights[1], conv_biases[1])
    residual = inputs + branch
    normed_three, inverse_three, pre_three = norm_forward(
        residual, norm_gains[2], norm_shifts[2], members
    )
    attn_input = pre_three.astype(jnp.bfloat16)
    mixed = jnp.dot(attn_input, qkv_weight, preferred_element_type=jnp.float32)
    queries = (mixed[:, :channels] + qv_bias[0]).astype(jnp.bfloat16)
    key_rows = mixed[:, channels : 2 * channels].astype(jnp.bfloat16)
    value_rows = (mixed[:, 2 * channels :] + qv_bias[1]).astype(jnp.bfloat16)
    running_max = jnp.full((pixels,), masked_score, jnp.float32)
    key_piece = lax.all_gather(key_rows, "height", axis=0, tiled=True)
    value_piece = lax.all_gather(value_rows, "height", axis=0, tiled=True)
    scores = (
        lax.dot_general(
            queries, key_piece, (((1,), (1,)), ((), ())), preferred_element_type=jnp.float32
        )
        * score_scale
    )
    same_tile = query_ids[:, None] == key_ids[None, :]
    scores = jnp.where(same_tile, scores, masked_score)
    new_max = jnp.maximum(running_max, jnp.max(scores, axis=1))
    weights = jnp.where(same_tile, jnp.exp(scores - new_max[:, None]), 0.0)
    summed_out = jnp.dot(
        weights.astype(jnp.bfloat16), value_piece, preferred_element_type=jnp.float32
    )
    total_weight = jnp.sum(weights, axis=1)
    log_total = new_max + jnp.log(total_weight)
    attended = summed_out / total_weight[:, None]
    attended_low = attended.astype(jnp.bfloat16)
    output = (
        residual
        + jnp.dot(attended_low, proj_weight, preferred_element_type=jnp.float32)
        + proj_bias
    )
    out_grad = cotangent[0].reshape(pixels, channels)
    out_grad_full = out_grad.astype(jnp.float32)
    proj_grad = lax.dot_general(
        attended_low, out_grad, (((0,), (0,)), ((), ())), preferred_element_type=jnp.float32
    )
    proj_bias_grad = jnp.sum(out_grad_full, axis=0)
    attended_grad = lax.dot_general(
        out_grad, proj_weight, (((1,), (1,)), ((), ())), preferred_element_type=jnp.float32
    ).astype(jnp.bfloat16)
    row_dots = jnp.sum(attended_grad.astype(jnp.float32) * attended, axis=1)
    block_rows = pixels * min(height_size, 8)
    zero_block = jnp.zeros((pixels, channels), jnp.float32)
    key_all, value_all = (
        lax.all_gather(key_rows, "height", axis=0, tiled=True),
        lax.all_gather(value_rows, "height", axis=0, tiled=True),
    )
    query_all, grad_all = (
        lax.all_gather(queries, "height", axis=0, tiled=True),
        lax.all_gather(attended_grad, "height", axis=0, tiled=True),
    )
    total_all, dots_all = (
        lax.all_gather(log_total, "height", axis=0, tiled=True),
        lax.all_gather(row_dots, "height", axis=0, tiled=True),
    )

    def own_query_step(running, block_index):
        offset = block_index * block_rows
        key_part = take_rows(key_all, offset, block_rows)
        rounded, score_grad = score_grads(
            queries,
            attended_grad,
            log_total,
            row_dots,
            query_ids,
            key_part,
            take_rows(value_all, offset, block_rows),
            take_rows(key_ids, offset, block_rows),
            score_scale,
        )
        return (
            running
            + jnp.dot(score_grad, key_part, preferred_element_type=jnp.float32) * score_scale,
            None,
        )

    def own_key_step(running, block_index):
        offset = block_index * block_rows
        query_part = take_rows(query_all, offset, block_rows)
        grad_part = take_rows(grad_all, offset, block_rows)
        rounded, score_grad = score_grads(
            query_part,
            grad_part,
            take_rows(total_all, offset, block_rows),
            take_rows(dots_all, offset, block_rows),
            take_rows(key_ids, offset, block_rows),
            key_rows,
            value_rows,
            query_ids,
            score_scale,
        )
        key_part = (
            lax.dot_general(
                score_grad, query_part, (((0,), (0,)), ((), ())), preferred_element_type=jnp.float32
            )
            * score_scale
        )
        value_part = lax.dot_general(
            rounded, grad_part, (((0,), (0,)), ((), ())), preferred_element_type=jnp.float32
        )
        return ((running[0] + key_part, running[1] + value_part), None)

    block_count = key_all.shape[0] // block_rows
    query_grad, unused_one = lax.scan(own_query_step, zero_block, jnp.arange(block_count))
    (key_grad, value_grad), unused_two = lax.scan(
        own_key_step, (zero_block, zero_block), jnp.arange(block_count)
    )
    query_low = query_grad.astype(jnp.bfloat16)
    key_low = key_grad.astype(jnp.bfloat16)
    value_low = value_grad.astype(jnp.bfloat16)
    stacked_grad = jnp.concatenate([query_low, key_low, value_low], axis=1)
    qkv_grad = lax.dot_general(
        attn_input, stacked_grad, (((0,), (0,)), ((), ())), preferred_element_type=jnp.float32
    )
    qv_grad = jnp.stack(
        [
            jnp.sum(query_low.astype(jnp.float32), axis=0),
            jnp.sum(value_low.astype(jnp.float32), axis=0),
        ]
    )
    normed_grad = lax.dot_general(
        stacked_grad, qkv_weight, (((1,), (1,)), ((), ())), preferred_element_type=jnp.float32
    )
    back_three, gain_three, shift_three = norm_backward(
        normed_grad, normed_three, inverse_three, norm_gains[2], members
    )
    residual_grad = out_grad_full + back_three
    grad_two = residual_grad.astype(jnp.bfloat16).reshape(grid_shape)
    act_two_grad, weight_two_grad, bias_two_grad = conv_backward(
        grad_two, row_mask, conv_weights[1], taps_two
    )
    middle_grad, gain_two, shift_two = norm_backward(
        act_two_grad * swish_slope(pre_two), normed_two, inverse_two, norm_gains[1], members
    )
    grad_one = middle_grad.astype(jnp.bfloat16).reshape(grid_shape)
    act_one_grad, weight_one_grad, bias_one_grad = conv_backward(
        grad_one, row_mask, conv_weights[0], taps_one
    )
    input_back, gain_one, shift_one = norm_backward(
        act_one_grad * swish_slope(pre_one), normed_one, inverse_one, norm_gains[0], members
    )
    input_grad = residual_grad + input_back
    conv_grad = jnp.stack([weight_one_grad, weight_two_grad])
    conv_part = lax.psum_scatter(conv_grad, "height", scatter_dimension=4, tiled=True)
    conv_part = lax.psum_scatter(
        conv_part.astype(jnp.bfloat16), "canvas", scatter_dimension=3, tiled=True
    ).astype(jnp.float32)
    summed = lax.psum(
        (
            jnp.stack([gain_one, gain_two, gain_three]),
            jnp.stack([shift_one, shift_two, shift_three]),
            jnp.stack([bias_one_grad, bias_two_grad]),
            qkv_grad,
            qv_grad,
            proj_grad,
            proj_bias_grad,
        ),
        ("canvas", "height"),
    )
    return (
        output.astype(jnp.bfloat16).reshape((1,) + grid_shape),
        input_grad.astype(jnp.bfloat16).reshape((1,) + grid_shape),
        summed[0],
        summed[1],
        conv_part,
        summed[2],
        summed[3],
        summed[4],
        summed[5],
        summed[6],
    )


def fold(block):
    rows, width = block.shape
    return jnp.sum(block.reshape(rows // 8, 8, width), axis=0)


def group_lanes(block, group):
    lane = lax.broadcasted_iota(jnp.int32, block.shape, 1)
    width = block.shape[1]
    step = 1
    while step < group:
        above = pltpu.roll(block, step, 1)
        below = pltpu.roll(block, width - step, 1)
        block = block + jnp.where((lane & step) != 0, above, below)
        step *= 2
    return block


def group_mean(partial, members):
    spread = group_lanes(partial, partial.shape[1] // GROUPS)
    return jnp.sum(spread, axis=0, keepdims=True) * (1.0 / members)


def widen(block, width):
    return jnp.concatenate([block] * (width // block.shape[1]), axis=1)


def each_block(pixels, block, body, carry=0):
    def step(index, carry):
        return body(pl.ds(pl.multiple_of(index * block, block), block), carry)

    return lax.fori_loop(0, pixels // block, step, carry)


def each_chunk(pixels, body, carry):
    return each_block(pixels, CHUNK, body, carry)


def aligned(start, step):
    return start if isinstance(start, int) else pl.multiple_of(start, step)


class RunningStats:
    def __init__(self, channels):
        self.width = channels // GROUPS
        self.reference = None
        self.sums = self.squares = jnp.zeros((8, channels), jnp.float32)

    def add(self, block):
        if self.reference is None:
            self.reference = group_mean(block[0:8], 8.0 * self.width)
        offset = block - self.reference
        self.sums = self.sums + fold(offset)
        self.squares = self.squares + fold(offset * offset)

    def finish(self, pixels):
        both = group_lanes(jnp.concatenate([self.sums, self.squares], axis=0), self.width)
        share = 1.0 / (pixels * self.width)
        offset = column_total(both[0:8]) * share
        variance = column_total(both[8:16]) * share - offset * offset
        return self.reference + offset, lax.rsqrt(jnp.maximum(variance, 0.0) + epsilon)


def put_taps(taps_ref, block, rows, cols):
    count, channels = block.shape
    place = lax.broadcasted_iota(jnp.int32, block.shape, 0) & (cols - 1)
    left = jnp.where(place == 0, 0.0, pltpu.roll(block, 1, 0))
    right = jnp.where(place == cols - 1, 0.0, pltpu.roll(block, count - 1, 0))
    inner = pl.ds(aligned(rows.start + cols, cols), count)
    taps_ref[inner, 0:channels] = left.astype(jnp.bfloat16)
    taps_ref[inner, channels : 2 * channels] = block.astype(jnp.bfloat16)
    taps_ref[inner, 2 * channels :] = right.astype(jnp.bfloat16)


def clear_edges(taps_ref, cols):
    edge = jnp.zeros((cols, taps_ref.shape[1]), taps_ref.dtype)
    taps_ref[0:cols, :] = edge
    taps_ref[taps_ref.shape[0] - cols :, :] = edge


def begin_conv(taps_ref, product, total_ref, fill, first, cols):
    for start in range(0, total_ref.shape[0], FILL_ROWS):
        for inner in range(start, start + FILL_ROWS, CHUNK):
            fill(pl.ds(inner, CHUNK))
        rows = pl.ds(start, FILL_ROWS)
        total_ref[rows, :] = first(rows, product(taps_ref, pl.ds(start + cols, FILL_ROWS), 1))


def add_rows(taps_ref, product, mask_ref, total_ref, stop, cols):
    rows = pl.ds(0, stop)
    part = product(taps_ref, rows, 0)
    total_ref[rows, :] += widen(mask_ref[0, rows, :], total_ref.shape[1]) * part


def end_conv(taps_ref, product, mask_ref, total_ref, last, cols, old_ref=None, pending=None):
    pixels, channels = total_ref.shape
    old_ref = total_ref if old_ref is None else old_ref
    pending = pixels if pending is None else pending
    for start in range(0, pixels, FILL_ROWS):
        rows = pl.ds(start, FILL_ROWS)
        value = old_ref[rows, :]
        for row_tap in (0, 2) if start >= pending else (2,):
            part = product(taps_ref, pl.ds(start + row_tap * cols, FILL_ROWS), row_tap)
            value = value + widen(mask_ref[row_tap // 2, rows, :], channels) * part
        total_ref[rows, :] = last(rows, value)


def run_conv(taps_ref, product, mask_ref, total_ref, fill, first, last, cols):
    begin_conv(taps_ref, product, total_ref, fill, first, cols)
    add_rows(taps_ref, product, mask_ref, total_ref, total_ref.shape[0], cols)
    end_conv(taps_ref, product, mask_ref, total_ref, last, cols)


def product_forward(weight_ref):
    channels = weight_ref.shape[-1]

    def product(taps_ref, shifted, row_tap):
        return jnp.dot(
            taps_ref[shifted, :],
            weight_ref[row_tap].reshape(3 * channels, channels),
            preferred_element_type=jnp.float32,
        )

    return product


def product_backward(weight_ref):
    def product(taps_ref, shifted, row_tap):
        return lax.dot_general(
            taps_ref[shifted, :],
            weight_ref[row_tap],
            (((1,), (1,)), ((), ())),
            preferred_element_type=jnp.float32,
        )

    return product


def activation(read, mean, inverse, gain, shift, act_ref, taps_ref, cols):
    scale, offset = 0.5 * inverse * gain, 0.5 * shift

    def fill(rows):
        half = (read(rows) - mean) * scale + offset
        act = half * (1.0 + jnp.tanh(half))
        act_ref[rows, :] = act.astype(jnp.bfloat16)
        put_taps(taps_ref, act, rows, cols)

    return fill


def back_means(sums, gain, pixels):
    channels = gain.shape[1]
    members = float(pixels * (channels // GROUPS))
    return group_mean(sums[0] * gain, members), group_mean(sums[1] * gain, members)


def column_total(partial):
    return jnp.sum(partial, axis=0, keepdims=True)


def weight_part(act_ref, narrow, lanes_ref, flip_ref, columns_ref, part_ref, cols):
    pixels, channels = act_ref.shape
    height = lax.axis_index("height")
    share = NARROW // 2
    flip_ref[...] = narrow.T
    own = pl.ds(pl.multiple_of((height % 2) * share, share), share)
    grad = flip_ref[own, :].astype(jnp.float32)
    column = lax.broadcasted_iota(jnp.int32, grad.shape, 1) & (cols - 1)
    for col_tap in range(3):
        shifted = grad
        if col_tap == 0:
            shifted = jnp.where(column == cols - 1, 0.0, pltpu.roll(grad, pixels - 1, 1))
        elif col_tap == 2:
            shifted = jnp.where(column == 0, 0.0, pltpu.roll(grad, 1, 1))
        for row_tap in range(3):
            tap = 3 * row_tap + col_tap
            place = slice(tap * share, (tap + 1) * share)
            if row_tap == 1:
                columns_ref[place, :] = shifted.astype(jnp.bfloat16)
                continue
            side, turn = (0, pixels - cols) if row_tap == 0 else (1, cols)
            masked = (shifted * lanes_ref[side : side + 1, :]).astype(jnp.bfloat16)
            columns_ref[place, :] = pltpu.roll(masked, turn, 1)
    part_ref[...] = jnp.dot(
        columns_ref[...], act_ref[...], preferred_element_type=jnp.float32
    ).astype(jnp.bfloat16)


def begin_back(read, weights_ref, mask_ref, taps_ref, total_ref, stop, cols):
    clear_edges(taps_ref, cols)

    def fill(rows):
        put_taps(taps_ref, read(rows), rows, cols)

    product = product_backward(weights_ref)
    begin_conv(taps_ref, product, total_ref, fill, lambda rows, part: part, cols)
    add_rows(taps_ref, product, mask_ref, total_ref, stop, cols)


def finish_back(
    weights_ref,
    mask_ref,
    taps_ref,
    total_ref,
    read,
    table_ref,
    which,
    cols,
    old_ref=None,
    pending=None,
):
    mean, inverse, gain, shift = norm_rows(table_ref, which)
    scale, offset = 0.5 * inverse * gain, 0.5 * shift
    sums = []

    def slope(rows, value):
        centered = read(rows) - mean
        half = centered * scale + offset
        turn = jnp.tanh(half)
        double = value * ((1.0 + turn) * (1.0 + half * (1.0 - turn)))
        sums.append((fold(double), fold(double * centered)))
        return double

    product = product_backward(weights_ref)
    end_conv(taps_ref, product, mask_ref, total_ref, slope, cols, old_ref, pending)
    plain, cross = sum(pair[0] for pair in sums), sum(pair[1] for pair in sums)
    return 0.5 * plain, 0.5 * inverse * cross


def norm_back(total_ref, double, sums, read, table_ref, which, pixels, scales_ref=None):
    mean, inverse, gain, shift = norm_rows(table_ref, which)
    mean_grad, mean_cross = back_means(sums, gain, pixels)
    slope = inverse * gain * (0.5 if double else 1.0)
    level, tilt = inverse * mean_grad, inverse * inverse * mean_cross
    if scales_ref is not None:
        for row, scales in enumerate((mean, slope, level, tilt)):
            scales_ref[row : row + 1, :] = scales

    def back(rows, inner):
        return total_ref[inner, :] * slope - level - (read(rows) - mean) * tilt

    return back


def own_lanes():
    block = lax.axis_index("height") // 2
    return pl.ds(pl.multiple_of(block * NARROW, NARROW), NARROW)


def narrow_back(total_ref, value_ref, scales_ref):
    lanes = own_lanes()
    mean, slope, level, tilt = (scales_ref[row : row + 1, lanes] for row in range(4))
    return total_ref[:, lanes] * slope - level - (value_ref[:, lanes] - mean) * tilt


def turn_kernel(grad_ref, mask_ref, weights_ref, total_ref, taps_ref, *, cols):
    def read(rows):
        return grad_ref[rows, :].astype(jnp.float32)

    begin_back(read, weights_ref.at[1], mask_ref, taps_ref, total_ref, EARLY_ROWS, cols)


def norm_rows(table_ref, which):
    picks = (2 * which, 2 * which + 1, 6 + which, 9 + which)
    return tuple(table_ref[pick : pick + 1, :] for pick in picks)


def build_masks(ids_ref, mask_ref, lanes_ref, id_rows_ref, id_cols_ref, cols):
    rows = ids_ref.shape[1]

    def one_row(row, carry):
        here = ids_ref[0, row]
        place = pl.ds(pl.multiple_of(row * cols, cols), cols)
        id_rows_ref[place, :] = jnp.full((cols, LANES), here, jnp.int32)
        for side, other in ((0, row - 1), (1, row + 1)):
            inside = jnp.logical_and(other >= 0, other < rows)
            other_id = ids_ref[0, jnp.clip(other, 0, rows - 1)]
            same = jnp.where(jnp.logical_and(inside, other_id == here), 1.0, 0.0)
            mask_ref[side, place, :] = jnp.full((cols, LANES), same, jnp.float32)
        return carry

    lax.fori_loop(0, rows, one_row, 0)
    lane = lax.broadcasted_iota(jnp.int32, (8, LANES), 1)
    each = LANES // cols
    for block in range(rows // each):
        ids = jnp.full((8, LANES), ids_ref[0, block * each], jnp.int32)
        for step in range(1, each):
            ids = jnp.where(lane >= step * cols, ids_ref[0, block * each + step], ids)
        id_cols_ref[:, block * LANES : (block + 1) * LANES] = ids
    ids = id_cols_ref[...].astype(jnp.float32)
    pixels = ids.shape[1]
    pixel = lax.broadcasted_iota(jnp.int32, ids.shape, 1)
    above = jnp.where(pixel < cols, -1.0, pltpu.roll(ids, cols, 1))
    below = jnp.where(pixel >= pixels - cols, -1.0, pltpu.roll(ids, pixels - cols, 1))
    lanes_ref[0:1, :] = jnp.where(above == ids, 1.0, 0.0)[0:1]
    lanes_ref[1:2, :] = jnp.where(below == ids, 1.0, 0.0)[0:1]


def place_pieces(pieces, whole_ref, sems):
    own_pixels = whole_ref.shape[0] // len(pieces)
    height = lax.axis_index("height")
    copies = []
    for place, piece in enumerate(pieces):
        piece = piece.at[piece.shape[0] - own_pixels : piece.shape[0], :]
        start = pl.multiple_of((height ^ place) * own_pixels, own_pixels)
        rows = pl.ds(start, own_pixels)
        copies.append(pltpu.make_async_copy(piece, whole_ref.at[rows, :], sems.at[place]))
    return copies


def hold_kernel(
    ids_hbm,
    gains_hbm,
    shifts_hbm,
    biases_hbm,
    weights_hbm,
    qkv_hbm,
    proj_hbm,
    qv_bias_hbm,
    proj_bias_hbm,
    weights_ref,
    turned_ref,
    qkv_ref,
    proj_ref,
    table_ref,
    mask_ref,
    lanes_ref,
    id_rows_ref,
    id_cols_ref,
    ids_ref,
    gains_ref,
    shifts_ref,
    biases_ref,
    qv_bias_ref,
    proj_bias_ref,
    sems,
    *,
    cols,
):
    channels = weights_ref.shape[-1]
    small = [
        (ids_hbm, ids_ref),
        (gains_hbm, gains_ref),
        (shifts_hbm, shifts_ref),
        (biases_hbm, biases_ref),
        (qv_bias_hbm, qv_bias_ref),
        (proj_bias_hbm, proj_bias_ref),
    ]
    large = [(weights_hbm, weights_ref), (qkv_hbm, qkv_ref), (proj_hbm, proj_ref)]
    for which in range(2):
        for row_tap in range(3):
            for col_tap in range(3):
                place = slice(col_tap * channels, (col_tap + 1) * channels)
                large.append(
                    (
                        weights_hbm.at[which, 2 - row_tap, 2 - col_tap],
                        turned_ref.at[which, row_tap, :, place],
                    )
                )
    copies = [
        pltpu.make_async_copy(source, target, sems.at[index])
        for index, (source, target) in enumerate(small + large)
    ]
    for copy in copies:
        copy.start()
    for copy in copies[: len(small)]:
        copy.wait()
    build_masks(ids_ref, mask_ref, lanes_ref, id_rows_ref, id_cols_ref, cols)
    table_ref[6:9, :] = gains_ref[...]
    table_ref[9:12, :] = shifts_ref[...]
    table_ref[12:14, :] = biases_ref[...]
    table_ref[14:16, :] = qv_bias_ref[...]
    table_ref[16:17, :] = proj_bias_ref[...]
    for copy in copies[len(small) :]:
        copy.wait()


def conv_kernel(*refs, cols, count):
    pieces, refs = refs[:count], refs[count:]
    (
        weights_ref,
        params_ref,
        mask_ref,
        features_ref,
        act_one_ref,
        middle_ref,
        act_two_ref,
        residual_ref,
        table_ref,
        own_ref,
        taps_ref,
        sem,
    ) = refs
    pixels, channels = features_ref.shape
    wide = jnp.float32
    own_copy = pltpu.make_async_copy(pieces[0], own_ref, sem)
    own_copy.start()
    table_ref[...] = params_ref[...]
    clear_edges(taps_ref, cols)

    def read_input(rows):
        return features_ref[rows, :].astype(wide)

    def read_middle(rows):
        return middle_ref[rows, :]

    height = lax.axis_index("height")
    own_pixels = pixels // count
    seen = RunningStats(channels)
    for place in list(range(1, count)) + [0]:
        if place == 0:
            own_copy.wait()
        piece = (pieces[place] if place else own_ref)[0:own_pixels, :]
        start = pl.multiple_of((height ^ place) * own_pixels, own_pixels)
        features_ref[pl.ds(start, own_pixels), :] = piece
        seen.add(piece.astype(wide))
    table_ref[0:1, :], table_ref[1:2, :] = seen.finish(pixels)
    seen = RunningStats(channels)

    def keep(rows, value):
        seen.add(value)
        return value

    run_conv(
        taps_ref,
        product_forward(weights_ref.at[0]),
        mask_ref,
        middle_ref,
        activation(read_input, *norm_rows(table_ref, 0), act_one_ref, taps_ref, cols),
        lambda rows, part: part + table_ref[12:13, :],
        keep,
        cols,
    )
    table_ref[2:3, :], table_ref[3:4, :] = seen.finish(pixels)
    seen = RunningStats(channels)
    run_conv(
        taps_ref,
        product_forward(weights_ref.at[1]),
        mask_ref,
        residual_ref,
        activation(read_middle, *norm_rows(table_ref, 1), act_two_ref, taps_ref, cols),
        lambda rows, part: part + (read_input(rows) + table_ref[13:14, :]),
        keep,
        cols,
    )
    table_ref[4:5, :], table_ref[5:6, :] = seen.finish(pixels)


def score_kernel(
    qkv_ref,
    proj_ref,
    residual_ref,
    table_ref,
    id_rows_ref,
    id_cols_ref,
    normed_ref,
    query_ref,
    key_ref,
    value_ref,
    soft_ref,
    out_flip_ref,
    output_ref,
    value_flip_ref,
    *scores_refs,
    score_scale,
):
    pixels, channels = residual_ref.shape
    own_pixels = output_ref.shape[0]
    wide = jnp.float32
    exponent = score_scale * 1.4426950408889634
    mean, inverse, gain, shift = norm_rows(table_ref, 2)
    scale = inverse * gain

    def normalise(start):
        rows = slice(start, start + KEY_ROWS)
        normed = (residual_ref[rows, :] - mean) * scale + shift
        normed_ref[rows, :] = normed.astype(jnp.bfloat16)

    def project(start):
        rows = slice(start, start + KEY_ROWS)
        normed = normed_ref[rows, :]
        query_ref[rows, :] = (
            jnp.dot(normed, qkv_ref[:, 0:channels], preferred_element_type=wide)
            + table_ref[14:15, :]
        ).astype(jnp.bfloat16)
        key_ref[rows, :] = jnp.dot(
            normed, qkv_ref[:, channels : 2 * channels], preferred_element_type=wide
        ).astype(jnp.bfloat16)
        values = (
            jnp.dot(normed, qkv_ref[:, 2 * channels :], preferred_element_type=wide)
            + table_ref[15:16, :]
        ).astype(jnp.bfloat16)
        value_ref[rows, :] = values
        value_flip_ref[:, rows] = values.T

    normalise(0)
    for start in range(0, pixels, KEY_ROWS):
        if start + KEY_ROWS < pixels:
            normalise(start + KEY_ROWS)
        project(start)
    block = scores_refs[0].shape[1]
    steps = range(0, pixels, KEY_ROWS)

    def score(index):
        rows = slice(index * block, (index + 1) * block)
        for start in steps:
            keys = slice(start, start + KEY_ROWS)
            scores = lax.dot_general(
                key_ref[keys, :],
                query_ref[rows, :],
                (((1,), (1,)), ((), ())),
                preferred_element_type=wide,
            )
            same = widen(id_rows_ref[keys, :], block) == id_cols_ref[0:1, rows]
            scores_refs[index][keys, :] = jnp.where(same, scores, masked_score)

    def soften(index):
        rows = slice(index * block, (index + 1) * block)
        scores_ref = scores_refs[index]
        peak = jnp.full((8, block), masked_score, wide)
        for start in steps:
            scores = scores_ref[start : start + KEY_ROWS, :]
            peak = jnp.maximum(peak, jnp.max(scores.reshape(-1, 8, block), axis=0))
        peak = jnp.max(peak, axis=0, keepdims=True)
        total = jnp.zeros((8, block), wide)
        for start in steps:
            keys = slice(start, start + KEY_ROWS)
            powers = jnp.exp2((scores_ref[keys, :] - peak) * exponent)
            scores_ref[keys, :] = powers
            total = total + fold(powers)
        share = 1.0 / column_total(total)
        for start in steps:
            keys = slice(start, start + KEY_ROWS)
            soft_ref[keys, rows] = (scores_ref[keys, :] * share).astype(jnp.bfloat16)

    score(0)
    for index in range(len(scores_refs)):
        if index + 1 < len(scores_refs):
            score(index + 1)
        soften(index)
        rows = slice(index * block, (index + 1) * block)
        out_flip_ref[:, rows] = jnp.dot(
            value_flip_ref[...], soft_ref[:, rows], preferred_element_type=wide
        ).astype(jnp.bfloat16)
    height = lax.axis_index("height")
    own = pl.ds(pl.multiple_of(height * own_pixels, own_pixels), own_pixels)
    output_ref[...] = (
        residual_ref[own, :]
        + lax.dot_general(
            out_flip_ref[:, own],
            proj_ref[...],
            (((0,), (0,)), ((), ())),
            preferred_element_type=wide,
        )
        + table_ref[16:17, :]
    ).astype(jnp.bfloat16)


def own_quarter():
    height = lax.axis_index("height")
    return (height & 1) * 2 + ((height >> 1) & 1)


def attention_kernel(
    proj_ref,
    normed_ref,
    query_ref,
    key_ref,
    value_ref,
    soft_ref,
    out_flip_ref,
    *refs,
    score_scale,
    count,
):
    pieces, (grad_ref, packed_ref, sums_ref), refs = (
        refs[:count],
        refs[count : count + 3],
        refs[count + 3 :],
    )
    pixels, channels = normed_ref.shape
    blocks = pixels // SCORE_ROWS
    grads_refs, refs = refs[-blocks:], refs[:-blocks]
    keep_ref, send_ref, mixed_ref, key_flip_ref, back_ref, score_grad_ref, flip_ref, sems = refs
    wide = jnp.float32
    copies = place_pieces(pieces, grad_ref, sems)
    for copy in copies:
        copy.start()
    quarter = channels // 4
    own = pl.ds(pl.multiple_of(own_quarter() * quarter, quarter), quarter)
    flip_ref[...] = normed_ref[:, own].T
    key_flip_ref[...] = key_ref[...].T
    for copy in copies:
        copy.wait()
    block, count = SCORE_ROWS, blocks
    steps = range(0, pixels, KEY_ROWS)

    def block_rows(index):
        return slice(index * block, (index + 1) * block)

    for index in range(count):
        back_ref[block_rows(index), :] = lax.dot_general(
            grad_ref[block_rows(index), :],
            proj_ref[...],
            (((1,), (1,)), ((), ())),
            preferred_element_type=wide,
        ).astype(jnp.bfloat16)

    def weigh(index):
        total = jnp.zeros((8, block), wide)
        for start in steps:
            keys = slice(start, start + KEY_ROWS)
            weight_grad = lax.dot_general(
                value_ref[keys, :],
                back_ref[block_rows(index), :],
                (((1,), (1,)), ((), ())),
                preferred_element_type=wide,
            )
            grads_refs[index][keys, :] = weight_grad
            total = total + fold(soft_ref[keys, block_rows(index)].astype(wide) * weight_grad)
        return column_total(total)

    def slope(index, dots):
        for start in steps:
            keys = slice(start, start + KEY_ROWS)
            weights = soft_ref[keys, block_rows(index)].astype(wide)
            score_grad_ref[keys, block_rows(index)] = (
                weights * (grads_refs[index][keys, :] - dots)
            ).astype(jnp.bfloat16)

    dots = weigh(0)
    for index in range(count):
        now, rows = dots, block_rows(index)
        if index + 1 < count:
            dots = weigh(index + 1)
        slope(index, now)
        packed_ref[rows, 2 * channels :] = jnp.dot(
            soft_ref[rows, :], back_ref[...], preferred_element_type=wide
        ).astype(jnp.bfloat16)
        query_grad = jnp.dot(
            key_flip_ref[...], score_grad_ref[:, rows], preferred_element_type=wide
        )
        packed_ref[rows, 0:channels] = (query_grad * score_scale).astype(jnp.bfloat16).T
    for index in range(count):
        rows = block_rows(index)
        packed_ref[rows, channels : 2 * channels] = (
            jnp.dot(score_grad_ref[rows, :], query_ref[...], preferred_element_type=wide)
            * score_scale
        ).astype(jnp.bfloat16)

    def pack(rows, carry):
        return (
            carry[0] + fold(packed_ref[rows, 0:channels].astype(wide)),
            carry[1] + fold(packed_ref[rows, 2 * channels :].astype(wide)),
            carry[2] + fold(grad_ref[rows, :].astype(wide)),
        )

    zeros = jnp.zeros((8, channels), wide)
    totals = zeros, zeros, zeros
    for start in range(0, pixels, CHUNK):
        totals = pack(pl.ds(start, CHUNK), totals)
    sums_ref[...] = jnp.zeros(sums_ref.shape, wide)
    for row, total in enumerate(totals):
        sums_ref[8 + row : 9 + row, :] = column_total(total)
    mixed_ref[:, 0 : 3 * channels] = jnp.dot(
        flip_ref[...], packed_ref[...], preferred_element_type=wide
    ).astype(jnp.bfloat16)
    mixed_ref[:, 3 * channels :] = jnp.dot(
        out_flip_ref[own, :], grad_ref[...], preferred_element_type=wide
    ).astype(jnp.bfloat16)
    keep_half(mixed_ref, 0, keep_ref, send_ref)


def third_kernel(
    qkv_ref,
    grad_ref,
    packed_ref,
    residual_ref,
    table_ref,
    act_two_ref,
    lanes_ref,
    old_sums_ref,
    residual_grad_ref,
    grad_two_ref,
    sums_ref,
    part_ref,
    total_ref,
    flip_ref,
    columns_ref,
    *,
    cols,
):
    pixels, channels = residual_ref.shape
    block = FILL_ROWS
    wide = jnp.float32
    mean, inverse, gain, shift = norm_rows(table_ref, 2)
    zeros = jnp.zeros((8, channels), wide)

    sums = (zeros, zeros)
    for start in range(0, pixels, block):
        rows = pl.ds(start, block)
        normed_grad = lax.dot_general(
            packed_ref[rows, :], qkv_ref[...], (((1,), (1,)), ((), ())), preferred_element_type=wide
        )
        total_ref[rows, :] = normed_grad
        centered = residual_ref[rows, :] - mean
        sums = sums[0] + fold(normed_grad), sums[1] + fold(normed_grad * centered)
    sums = sums[0], sums[1] * inverse
    sums_ref[...] = old_sums_ref[...]
    sums_ref[5:6, :] = column_total(sums[1])
    sums_ref[6:7, :] = column_total(sums[0])
    back = norm_back(
        total_ref, False, sums, lambda rows: residual_ref[rows, :], table_ref, 2, pixels
    )

    def finish(rows, carry):
        total = grad_ref[rows, :].astype(wide) + back(rows, rows)
        residual_grad_ref[rows, :] = total
        low = total.astype(jnp.bfloat16)
        grad_two_ref[rows, :] = low
        return carry + fold(low.astype(wide))

    sums_ref[7:8, :] = column_total(each_chunk(pixels, finish, zeros))
    narrow = grad_two_ref[:, own_lanes()]
    weight_part(act_two_ref, narrow, lanes_ref, flip_ref, columns_ref, part_ref, cols)


def second_kernel(
    old_total_ref,
    taps_ref,
    middle_ref,
    table_ref,
    act_one_ref,
    mask_ref,
    lanes_ref,
    weights_ref,
    old_sums_ref,
    part_two_ref,
    total_ref,
    scales_ref,
    sums_ref,
    keep_one_ref,
    send_one_ref,
    keep_two_ref,
    send_two_ref,
    flip_ref,
    columns_ref,
    part_ref,
    *,
    cols,
):
    pixels, channels = middle_ref.shape

    def read(rows):
        return middle_ref[rows, :]

    sums = finish_back(
        weights_ref.at[1],
        mask_ref,
        taps_ref,
        total_ref,
        read,
        table_ref,
        1,
        cols,
        old_total_ref,
        EARLY_ROWS,
    )
    norm_back(total_ref, True, sums, read, table_ref, 1, pixels, scales_ref)
    narrow = narrow_back(total_ref, middle_ref, scales_ref).astype(jnp.bfloat16)
    weight_part(act_one_ref, narrow, lanes_ref, flip_ref, columns_ref, part_ref, cols)
    sums_ref[...] = old_sums_ref[...]
    sums_ref[2:3, :] = column_total(sums[1])
    sums_ref[3:4, :] = column_total(sums[0])
    keep_half(part_ref, 1, keep_one_ref, send_one_ref)
    keep_half(part_two_ref, 1, keep_two_ref, send_two_ref)


def near_far():
    core = lax.axis_index("height") & 1
    return 1 + core, 2 - core


def keep_half(source_ref, axis, keep_ref, send_ref):
    me = lax.axis_index("canvas")
    near, far = near_far()
    rows, width = keep_ref.shape[0] // 2, keep_ref.shape[1]
    for target_ref, flip in ((keep_ref, 0), (send_ref, near)):
        for slot, other in enumerate((0, far)):
            owner = me ^ flip ^ other
            target = target_ref.at[slot * rows : (slot + 1) * rows, :]
            if axis == 0:
                target[...] = source_ref[pl.ds(pl.multiple_of(owner * rows, rows), rows), :]
            else:
                target[...] = source_ref[:, pl.ds(pl.multiple_of(owner * width, width), width)]


def first_kernel(
    total_two_ref,
    scales_ref,
    middle_ref,
    features_ref,
    table_ref,
    mask_ref,
    old_sums_ref,
    weights_ref,
    own_ref,
    sums_ref,
    partial_ref,
    total_ref,
    taps_ref,
    *,
    cols,
):
    def read(rows):
        return features_ref[rows, :].astype(jnp.float32)

    mean, slope, level, tilt = (scales_ref[row : row + 1, :] for row in range(4))
    grad_sums = []

    def read_grad(rows):
        grad = total_two_ref[rows, :] * slope - level - (middle_ref[rows, :] - mean) * tilt
        grad = grad.astype(jnp.bfloat16).astype(jnp.float32)
        grad_sums.append(fold(grad))
        return grad

    weights = weights_ref.at[0]
    begin_back(read_grad, weights, mask_ref, taps_ref, total_ref, total_ref.shape[0], cols)
    sums = finish_back(weights, mask_ref, taps_ref, total_ref, read, table_ref, 0, cols)
    partial_ref[0:8, :], partial_ref[8:16, :] = sums
    sums_ref[...] = old_sums_ref[...]
    sums_ref[0:1, :] = column_total(sums[1])
    sums_ref[1:2, :] = column_total(sums[0])
    sums_ref[4:5, :] = column_total(sum(grad_sums))
    count = own_ref.shape[0]
    own = pl.ds(pl.multiple_of(lax.axis_index("height") * count, count), count)
    own_ref[...] = total_ref[own, :]


def own_kernel(
    own_ref, partial_ref, features_ref, residual_grad_ref, table_ref, input_grad_ref
):
    def read(rows):
        return features_ref[rows, :].astype(jnp.float32)

    sums = partial_ref[0:8, :], partial_ref[8:16, :]
    pixels = features_ref.shape[0]
    back = norm_back(own_ref, True, sums, read, table_ref, 0, pixels)
    count = own_ref.shape[0]
    own = pl.ds(pl.multiple_of(lax.axis_index("height") * count, count), count)
    total = residual_grad_ref[own, :] + back(own, slice(0, count))
    input_grad_ref[...] = total.astype(jnp.bfloat16)


def place_kernel(*refs):
    joints, packed_ref = refs[:-1], refs[-1]
    share = packed_ref.shape[0] // len(joints)
    me = lax.axis_index("canvas")
    for step, joint in enumerate(joints):
        place = pl.ds(pl.multiple_of((me ^ step) * share, share), share)
        packed_ref[place, :] = joint[...]


def cut_kernel(packed_ref, *half_refs):
    rows = half_refs[0].shape[0]
    for index, half_ref in enumerate(half_refs):
        half_ref[...] = packed_ref[index * rows : (index + 1) * rows, :]


def spread_quarters(packed, flips, qkv_ref, proj_ref, qkv_hbm, proj_hbm, sems):
    quarter = packed[0].shape[0]
    inner = qkv_ref.shape[2]
    copies = []
    for index, packed_ref in enumerate(packed):
        owner = own_quarter() ^ flips[index]
        rows = pl.ds(pl.multiple_of(owner * quarter, quarter), quarter)
        qkv_ref[index] = packed_ref[:, 0:inner].astype(jnp.float32)
        proj_ref[index] = packed_ref[:, inner:].astype(jnp.float32)
        for which, (held, target) in enumerate(((qkv_ref, qkv_hbm), (proj_ref, proj_hbm))):
            copy = pltpu.make_async_copy(held.at[index], target.at[rows, :], sems.at[index, which])
            copy.start()
            copies.append(copy)
    return copies


def join_kernel(*refs):
    packed, (qkv_hbm, proj_hbm, qkv_ref, proj_ref, sems) = refs[:-5], refs[-5:]
    copies = spread_quarters(packed, [0, 2], qkv_ref, proj_ref, qkv_hbm, proj_hbm, sems)
    for copy in copies:
        copy.wait()


def halve_kernel(keep_ref, got_ref, hold_ref, send_ref):
    total = keep_ref[...].astype(jnp.float32) + got_ref[...].astype(jnp.float32)
    rows = hold_ref.shape[0]
    hold_ref[...] = total[0:rows]
    send_ref[0:rows, :] = total[rows:].astype(jnp.bfloat16)


def halve_both_kernel(
    keep_ref, got_ref, keep_two_ref, got_two_ref, hold_ref, send_ref, hold_two_ref
):
    rows = hold_ref.shape[0]
    halve_kernel(keep_ref, got_ref, hold_ref, send_ref)
    halve_kernel(keep_two_ref, got_two_ref, hold_two_ref, send_ref.at[rows : 2 * rows, :])


def last_kernel(
    chip_ref,
    both_a_ref,
    both_b_ref,
    old_qkv,
    old_proj,
    qkv_hbm,
    proj_hbm,
    qkv_ref,
    proj_ref,
    sems,
):
    copies = []
    rows = both_a_ref.shape[0]
    inner = qkv_ref.shape[2]
    chips = (chip_ref.at[0:rows, :], chip_ref.at[rows : 2 * rows, :])
    for index, piece_ref in enumerate((*chips, both_a_ref, both_b_ref)):
        start = ((own_quarter() ^ (1 if index < 2 else 3)) * 2 + index % 2) * rows
        target = pl.ds(pl.multiple_of(start, rows), rows)
        qkv_ref[index] = piece_ref[:, 0:inner].astype(jnp.float32)
        proj_ref[index] = piece_ref[:, inner:].astype(jnp.float32)
        for which, (held, whole) in enumerate(((qkv_ref, qkv_hbm), (proj_ref, proj_hbm))):
            copy = pltpu.make_async_copy(held.at[index], whole.at[target, :], sems.at[index, which])
            copy.start()
            copies.append(copy)
    for copy in copies:
        copy.wait()


def sums_kernel(
    sums_ref,
    got_sums_ref,
    hold_one_ref,
    hold_two_ref,
    got_ref,
    share_ref,
    gains_ref,
    shifts_ref,
    conv_ref,
    qv_ref,
    bias_ref,
):
    rows = hold_one_ref.shape[0]
    for which, hold_ref in enumerate((hold_one_ref, hold_two_ref)):
        got = got_ref[which * rows : (which + 1) * rows, :].astype(jnp.float32)
        share_ref[which] = (hold_ref[...] + got).reshape(share_ref.shape[1:])
    total = sums_ref[...] + got_sums_ref[...]
    for row, start in enumerate((0, 2, 5)):
        gains_ref[row : row + 1, :] = total[start : start + 1]
        shifts_ref[row : row + 1, :] = total[start + 1 : start + 2]
    conv_ref[0:1, :] = total[4:5]
    conv_ref[1:2, :] = total[7:8]
    qv_ref[...] = total[8:10]
    bias_ref[...] = total[10:11]


def call_kernel(kernel, outputs, scratch, operands, places, flops, limit, out_places=None, aliases={}):
    out_places = out_places or "v" * len(outputs)
    spaces = {
        "v": pl.BlockSpec(memory_space=pltpu.VMEM),
        "s": pl.BlockSpec(memory_space=pltpu.SMEM),
        "h": pl.BlockSpec(memory_space=pl.ANY),
        "o": pl.BlockSpec(memory_space=pltpu.VMEM),
        "a": pl.BlockSpec(memory_space=pl.ANY),
    }
    moved = 8 * flops // LANES
    held = {"v": pltpu.VMEM, "h": pltpu.HBM, "o": jax.ShapeDtypeStruct}
    operands = [
        pltpu.with_memory_space_constraint(array, pltpu.HBM) if place == "h" else array
        for array, place in zip(operands, places)
    ]
    return pl.pallas_call(
        kernel,
        out_shape=[held[place](*output) for output, place in zip(outputs, out_places)],
        in_specs=[spaces[place] for place in places],
        out_specs=[spaces[place] for place in out_places],
        scratch_shapes=scratch,
        input_output_aliases=aliases,
        compiler_params=pltpu.CompilerParams(vmem_limit_bytes=limit * 2**20),
        cost_estimate=pl.CostEstimate(flops=flops, bytes_accessed=moved, transcendentals=0),
    )(*operands)


def send_height(block, step):
    size = lax.axis_size("height")
    return lax.ppermute(block, "height", [(i, i ^ step) for i in range(size)])


def with_cores(blocks, other):
    pieces = [blocks[0], other]
    for block in blocks[1:]:
        pieces += [block, send_height(block, 1)]
    return pieces


def send_canvas(block, step):
    size = lax.axis_size("canvas")
    return lax.ppermute(block, "canvas", [(i, i ^ step) for i in range(size)])


def send_phase(block, phase):
    canvases, size = lax.axis_size("canvas"), lax.axis_size("height")
    pairs = []
    for canvas in range(canvases):
        for height in range(size):
            step = 2 if (height ^ phase) & 1 else 1
            pairs.append((canvas * size + height, (canvas ^ step) * size + height))
    return lax.ppermute(block, ("canvas", "height"), pairs)


def trade_canvas(pieces):
    return [pieces[0]] + [send_canvas(piece, step) for step, piece in enumerate(pieces) if step]


def whole_canvas(
    features,
    tile_ids,
    norm_gains,
    norm_shifts,
    conv_weights,
    conv_biases,
    qkv_weight,
    qv_bias,
    proj_weight,
    proj_bias,
    cotangent,
):
    height_size = lax.axis_size("height")
    canvas_size = lax.axis_size("canvas")
    local_rows, cols, channels = features.shape[1:]
    all_rows = tile_ids.shape[1]
    pixels = all_rows * cols
    own_pixels = local_rows * cols
    out_share = channels // height_size
    ci_share = channels // canvas_size
    quarter = channels // 4
    row_share = quarter // canvas_size
    low, wide = jnp.bfloat16, jnp.float32

    own_features = features.reshape(own_pixels, channels)
    own_grad = cotangent.reshape(own_pixels, channels)
    steps = range(2, height_size, 2)
    held_features = [own_features] + [send_height(own_features, step) for step in steps]
    plane = ((pixels, channels), low)
    plane_wide = ((pixels, channels), wide)
    sums_shape = ((16, channels), wide)
    mixed_halves = [((2 * row_share, 4 * channels), low)] * 2
    taps = pltpu.VMEM((pixels + 2 * cols, 3 * channels), low)
    held_wide = pltpu.VMEM((pixels, channels), wide)
    flipped = pltpu.VMEM((channels, pixels), low)
    narrow = pltpu.VMEM((NARROW, pixels), low)
    columns = pltpu.VMEM((9 * out_share, pixels), low)
    part_held = pltpu.VMEM((9 * out_share, channels), low)
    sem = pltpu.SemaphoreType.DMA
    conv_flops = 2 * 9 * pixels * channels * channels
    dot_flops = 2 * pixels * channels * channels
    score_flops = 2 * pixels * pixels * channels
    scale = channels ** (-0.5)

    (
        held_conv,
        turned,
        held_qkv,
        held_proj,
        params,
        mask,
        lane_mask,
        id_rows,
        id_cols,
    ) = call_kernel(
        functools.partial(hold_kernel, cols=cols),
        [
            (conv_weights.shape, low),
            ((2, 3, channels, 3 * channels), low),
            (qkv_weight.shape, low),
            (proj_weight.shape, low),
            ((24, channels), wide),
            ((2, pixels, LANES), wide),
            ((8, pixels), wide),
            ((pixels, LANES), jnp.int32),
            ((8, pixels), jnp.int32),
        ],
        [
            pltpu.SMEM(tile_ids.shape, jnp.int32),
            pltpu.VMEM(norm_gains.shape, wide),
            pltpu.VMEM(norm_shifts.shape, wide),
            pltpu.VMEM(conv_biases.shape, wide),
            pltpu.VMEM(qv_bias.shape, wide),
            pltpu.VMEM((1, channels), wide),
            sem((27,)),
        ],
        [
            tile_ids,
            norm_gains,
            norm_shifts,
            conv_biases,
            conv_weights,
            qkv_weight,
            proj_weight,
            qv_bias,
            proj_bias.reshape(1, channels),
        ],
        "h" * 9,
        conv_flops,
        8,
    )
    held_features[1:] = [
        lax.optimization_barrier((params, block))[1] for block in held_features[1:]
    ]
    other_core = send_height(jnp.concatenate([own_features, own_grad], axis=0), 1)
    pieces = with_cores(held_features, other_core)
    far_grad, *pieces[4::2] = lax.optimization_barrier((own_grad, *held_features[2:]))
    held_grads = [own_grad, send_height(own_grad, 2)]
    held_grads[1], pieces[2] = lax.optimization_barrier((held_grads[1], held_features[1]))
    held_grads += [send_height(far_grad, step) for step in steps[1:]]

    all_features, act_one, middle, act_two, residual, table = call_kernel(
        functools.partial(conv_kernel, cols=cols, count=height_size),
        [plane, plane, plane_wide, plane, plane_wide, ((24, channels), wide)],
        [pltpu.VMEM((own_pixels, channels), low), taps, sem],
        [*pieces, held_conv, params, mask],
        "h" + "v" * (height_size + 2),
        2 * conv_flops,
        16,
    )
    residual, *held_grads = lax.optimization_barrier((residual, *held_grads))
    grad_pieces = with_cores(held_grads, other_core)
    normed, query, key, value, soft, out_flip, output = call_kernel(
        functools.partial(score_kernel, score_scale=scale),
        [
            plane,
            plane,
            plane,
            plane,
            ((pixels, pixels), low),
            ((channels, pixels), low),
            ((own_pixels, channels), low),
        ],
        [
            flipped,
            *[pltpu.VMEM((pixels, SCORE_ROWS), wide)] * (pixels // SCORE_ROWS),
        ],
        [
            held_qkv,
            held_proj,
            residual,
            table,
            id_rows,
            id_cols,
        ],
        "vvvvvv",
        3 * dot_flops + 2 * score_flops,
        20,
        "v" * 6 + "o",
    )
    normed, *grad_pieces = lax.optimization_barrier((normed, *grad_pieces))
    all_grad, packed, sums, keep_mixed, send_mixed = call_kernel(
        functools.partial(attention_kernel, score_scale=scale, count=height_size),
        [plane, ((pixels, 3 * channels), low), sums_shape, *mixed_halves],
        [
            pltpu.VMEM((quarter, 4 * channels), low),
            flipped,
            pltpu.VMEM((pixels, channels), low),
            pltpu.VMEM((pixels, pixels), low),
            pltpu.VMEM((quarter, pixels), low),
            sem((height_size,)),
            *[pltpu.VMEM((pixels, SCORE_ROWS), wide)] * (pixels // SCORE_ROWS),
        ],
        [held_proj, normed, query, key, value, soft, out_flip, *grad_pieces],
        "vvvvvvvh" + "a" * (height_size - 1),
        3 * dot_flops + 4 * score_flops,
        20,
    )
    got_mixed = send_phase(send_mixed, 0)
    residual_grad, grad_two, sums, part_two = call_kernel(
        functools.partial(third_kernel, cols=cols),
        [plane_wide, plane, sums_shape, ((9 * out_share, channels), low)],
        [held_wide, narrow, columns],
        [held_qkv, all_grad, packed, residual, table, act_two, lane_mask, sums],
        "vvvvvvvv",
        3 * dot_flops + conv_flops // height_size,
        16,
    )
    grad_two, got_mixed = lax.optimization_barrier((grad_two, got_mixed))
    hold_mixed, send_mixed = call_kernel(
        halve_kernel,
        [((row_share, 4 * channels), kind) for kind in (wide, low)],
        [],
        [keep_mixed, got_mixed],
        "vv",
        1,
        12,
    )
    got_mixed = send_phase(send_mixed, 1)
    grad_two, hold_mixed = lax.optimization_barrier((grad_two, hold_mixed))
    half_total, half_taps = call_kernel(
        functools.partial(turn_kernel, cols=cols),
        [plane_wide, (taps.shape, low)],
        [],
        [grad_two, mask, turned],
        "vvv",
        2 * conv_flops // 3,
        16,
    )
    half_total, got_mixed = lax.optimization_barrier((half_total, got_mixed))
    mixed_sum = (hold_mixed + got_mixed.astype(wide)).astype(low)
    joints = trade_canvas([mixed_sum] * canvas_size)
    halves = [((2 * 9 * out_share, ci_share), low)] * 4
    total_two, scales, sums, keep_one, send_one, keep_two, send_two = call_kernel(
        functools.partial(second_kernel, cols=cols),
        [plane_wide, ((8, channels), wide), sums_shape, *halves],
        [narrow, columns, part_held],
        [half_total, half_taps, middle, table, act_one, mask, lane_mask, turned, sums, part_two],
        "v" * 10,
        conv_flops // 2,
        20,
    )
    total_two, *joints = lax.optimization_barrier((total_two, *joints))
    (own_mixed,) = call_kernel(
        place_kernel,
        [((quarter, 4 * channels), low)],
        [],
        joints,
        "v" * canvas_size,
        1,
        12,
    )
    own_mixed, send_one, send_two = lax.optimization_barrier((own_mixed, send_one, send_two))
    chip_mixed = send_height(own_mixed, 2)
    core_mixed = send_height(own_mixed, 1)
    got_one, got_two = send_phase(send_one, 0), send_phase(send_two, 0)
    own_total, sums, partial_sums = call_kernel(
        functools.partial(first_kernel, cols=cols),
        [((own_pixels, channels), wide), sums_shape, sums_shape],
        [held_wide, taps],
        [total_two, scales, middle, all_features, table, mask, sums, turned],
        "vvvvvvvv",
        1,
        20,
    )
    got_sums, own_sums = send_phase(sums, 0), sums
    sums, core_mixed, got_one, got_two = lax.optimization_barrier(
        (sums, core_mixed, got_one, got_two)
    )
    share_rows = 9 * out_share
    hold_one, send_share, hold_two = call_kernel(
        halve_both_kernel,
        [
            ((share_rows, ci_share), wide),
            ((2 * share_rows, ci_share), low),
            ((share_rows, ci_share), wide),
        ],
        [],
        [keep_one, got_one, keep_two, got_two],
        "vvvv",
        1,
        12,
    )
    got_share = send_phase(send_share, 1)

    def widened(count, rows):
        return [
            pltpu.VMEM((count, rows, 3 * channels), wide),
            pltpu.VMEM((count, rows, channels), wide),
            sem((count, 2)),
        ]

    grad_shapes = [(qkv_weight.shape, wide), (proj_weight.shape, wide)]
    core_mixed, hold_one = lax.optimization_barrier((core_mixed, hold_one))
    qkv_grad, proj_grad = call_kernel(
        join_kernel,
        grad_shapes,
        widened(2, quarter),
        [own_mixed, core_mixed],
        "vv",
        1,
        12,
        "hh",
    )
    qkv_grad, chip_mixed, got_sums = lax.optimization_barrier((qkv_grad, chip_mixed, got_sums))
    sums = own_sums + got_sums
    got_sums = send_phase(sums, 1)
    chip_halves = call_kernel(
        cut_kernel,
        [((quarter // 2, 4 * channels), low)] * 2,
        [],
        [chip_mixed],
        "v",
        1,
        12,
    )
    both_halves = [send_height(half, 1) for half in chip_halves]
    qkv_grad, proj_grad = call_kernel(
        last_kernel,
        grad_shapes,
        widened(4, quarter // 2),
        [chip_mixed, *both_halves, qkv_grad, proj_grad],
        "vvvhh",
        1,
        12,
        "hh",
        {3: 0, 4: 1},
    )
    qkv_grad, own_total = lax.optimization_barrier((qkv_grad, own_total))
    (input_grad,) = call_kernel(
        own_kernel,
        [((own_pixels, channels), low)],
        [],
        [own_total, partial_sums, all_features, residual_grad, table],
        "vvvvv",
        dot_flops // 4,
        12,
        "o",
    )
    input_grad, got_share, got_sums = lax.optimization_barrier((input_grad, got_share, got_sums))
    vector_shapes = [norm_gains.shape, norm_shifts.shape, conv_biases.shape, qv_bias.shape]
    conv_grad, gains_grad, shifts_grad, biases_grad, qv_grad, proj_bias_grad = call_kernel(
        sums_kernel,
        [((2, 3, 3, out_share, ci_share), wide)]
        + [(shape, wide) for shape in vector_shapes + [(1, channels)]],
        [],
        [sums, got_sums, hold_one, hold_two, got_share],
        "vvvvv",
        1,
        12,
        "o" * 6,
    )
    own_shape = (1, local_rows, cols, channels)
    return (
        output.reshape(own_shape),
        input_grad.reshape(own_shape),
        gains_grad,
        shifts_grad,
        jnp.swapaxes(conv_grad, 3, 4),
        biases_grad,
        qkv_grad,
        qv_grad,
        proj_grad,
        proj_bias_grad.reshape(channels),
    )


def on_device(*arrays):
    features, tile_ids = arrays[0], arrays[1]
    local_rows, cols, channels = features.shape[1:]
    pixels = tile_ids.shape[1] * cols
    height_size, canvas_size = lax.axis_size("height"), lax.axis_size("canvas")
    powers = all(size & (size - 1) == 0 for size in (height_size, canvas_size, cols))
    fits = (
        powers
        and height_size > 2
        and canvas_size == 4
        and channels == LANES * canvas_size
        and pixels <= MOST_PIXELS
        and pixels % FILL_ROWS == 0
        and pixels >= EARLY_ROWS
        and FILL_ROWS % CHUNK == 0
        and pixels % SCORE_ROWS == 0
        and pixels % KEY_ROWS == 0
        and (local_rows * cols) % LANES == 0
        and CHUNK % cols == 0
        and cols % 16 == 0
        and channels % (LANES * canvas_size) == 0
        and 2 * channels == NARROW * height_size
    )
    return whole_canvas(*arrays) if fits else split_canvas(*arrays)


def solution(mesh):
    in_specs = (
        P("canvas", "height", None, None),
        P("canvas", None),
        P(),
        P(),
        P(),
        P(),
        P(),
        P(),
        P(),
        P(),
        P("canvas", "height", None, None),
    )
    out_specs = (
        P("canvas", "height", None, None),
        P("canvas", "height", None, None),
        P(),
        P(),
        P(None, None, None, "canvas", "height"),
        P(),
        P(),
        P(),
        P(),
        P(),
    )
    return jax.shard_map(
        on_device, mesh=mesh, in_specs=in_specs, out_specs=out_specs, check_vma=False
    )
```

```python
import functools

import jax
import jax.numpy as jnp
from jax import lax
from jax.experimental import pallas as pl
from jax.experimental.pallas import tpu as pltpu
from jax.sharding import PartitionSpec as P

GROUPS = 32


epsilon = 1e-06
masked_score = -1e30
MOST_PIXELS = 1024
LANES = 128
NARROW = 128
CHUNK = 128
FILL_ROWS = 256
EARLY_ROWS = 0
SCORE_ROWS = 256
KEY_ROWS = 256


def extended(block, sides, width):
    for axis, dim in sides:
        count = lax.axis_size(axis)
        forward = [(i, i + 1) for i in range(count - 1)]
        backward = [(target, source) for source, target in forward]
        low = lax.ppermute(
            lax.slice_in_dim(block, block.shape[dim] - width, None, axis=dim), axis, forward
        )
        high = lax.ppermute(lax.slice_in_dim(block, 0, width, axis=dim), axis, backward)
        block = jnp.concatenate([low, block, high], axis=dim)
    return block


def group_total(vector):
    return vector.reshape(GROUPS, -1).sum(axis=1)


def spread_groups(vector, channels):
    return jnp.repeat(vector, channels // GROUPS)


def norm_forward(values, gain, shift, members):
    channels = values.shape[1]
    totals = lax.psum(group_total(jnp.sum(values, axis=0)), "height")
    centered = values - spread_groups(totals / members, channels)
    squares = lax.psum(group_total(jnp.sum(centered * centered, axis=0)), "height")
    inverse = spread_groups(lax.rsqrt(squares / members + epsilon), channels)
    normed = centered * inverse
    return (normed, inverse, normed * gain + shift)


def norm_backward(grad_in, normed, inverse, gain, members):
    channels = grad_in.shape[1]
    scaled = grad_in * gain
    both_sums = lax.psum(
        (group_total(jnp.sum(scaled, axis=0)), group_total(jnp.sum(scaled * normed, axis=0))),
        "height",
    )
    mean_grad = spread_groups(both_sums[0] / members, channels)
    mean_cross = spread_groups(both_sums[1] / members, channels)
    result = inverse * (scaled - mean_grad - normed * mean_cross)
    return (result, jnp.sum(grad_in * normed, axis=0), jnp.sum(grad_in, axis=0))


def swish(values):
    return values * jax.nn.sigmoid(values)


def swish_slope(values):
    sigmoid_part = jax.nn.sigmoid(values)
    return sigmoid_part * (1.0 + values * (1.0 - sigmoid_part))


def tap_columns(padded, row_mask, local_rows, canvas_cols):
    pieces = []
    for row_tap in range(3):
        rows_taken = padded[row_tap : row_tap + local_rows] * row_mask[:, row_tap, None, None]
        for col_tap in range(3):
            pieces.append(rows_taken[:, col_tap : col_tap + canvas_cols])
    stacked = jnp.concatenate(pieces, axis=2)
    return stacked.reshape(local_rows * canvas_cols, stacked.shape[2])


def conv_forward(acts, row_mask, weight, bias):
    local_rows, canvas_cols, channels = acts.shape
    rimmed = extended(acts, (("height", 0),), 1)
    padded = jnp.pad(rimmed, ((0, 0), (1, 1), (0, 0)))
    gathered = tap_columns(padded, row_mask, local_rows, canvas_cols)
    result = (
        jnp.dot(
            gathered, weight.reshape(9 * channels, channels), preferred_element_type=jnp.float32
        )
        + bias
    )
    return (result, gathered)


def conv_backward(grad_low, row_mask, weight, gathered):
    local_rows, canvas_cols, channels = grad_low.shape
    flat_grad = grad_low.reshape(local_rows * canvas_cols, channels)
    weight_grad = lax.dot_general(
        gathered, flat_grad, (((0,), (0,)), ((), ())), preferred_element_type=jnp.float32
    )
    rimmed = extended(grad_low, (("height", 0),), 1)
    padded = jnp.pad(rimmed, ((0, 0), (1, 1), (0, 0)))
    grad_taps = tap_columns(padded, row_mask, local_rows, canvas_cols)
    flipped = jnp.transpose(weight[::-1, ::-1], (0, 1, 3, 2)).reshape(9 * channels, channels)
    input_part = jnp.dot(grad_taps, flipped, preferred_element_type=jnp.float32)
    return (
        input_part,
        weight_grad.reshape(3, 3, channels, channels),
        jnp.sum(flat_grad.astype(jnp.float32), axis=0),
    )


def take_rows(array, offset, count):
    return lax.dynamic_slice_in_dim(array, offset, count)


def score_grads(
    queries, out_grad, log_total, row_dots, query_ids, key_rows, value_rows, key_ids, score_scale
):
    scores = (
        lax.dot_general(
            queries, key_rows, (((1,), (1,)), ((), ())), preferred_element_type=jnp.float32
        )
        * score_scale
    )
    same_tile = query_ids[:, None] == key_ids[None, :]
    softmax_block = jnp.exp(jnp.where(same_tile, scores - log_total[:, None], masked_score))
    weight_grad = lax.dot_general(
        out_grad, value_rows, (((1,), (1,)), ((), ())), preferred_element_type=jnp.float32
    )
    score_grad = (softmax_block * (weight_grad - row_dots[:, None])).astype(jnp.bfloat16)
    return (softmax_block.astype(jnp.bfloat16), score_grad)


def split_canvas(
    features,
    tile_ids,
    norm_gains,
    norm_shifts,
    conv_weights,
    conv_biases,
    qkv_weight,
    qv_bias,
    proj_weight,
    proj_bias,
    cotangent,
):
    height_size = lax.axis_size("height")
    local_rows = features.shape[1]
    canvas_cols = features.shape[2]
    channels = features.shape[3]
    pixels = local_rows * canvas_cols
    row_ids = tile_ids[0]
    all_rows = row_ids.shape[0]
    members = float(all_rows * canvas_cols * (channels // GROUPS))
    score_scale = channels ** (-0.5)
    first_row = lax.axis_index("height") * local_rows
    edge_ids = jnp.full((1,), -1, jnp.int32)
    padded_ids = jnp.concatenate([edge_ids, row_ids, edge_ids])
    near_ids = lax.dynamic_slice_in_dim(padded_ids, first_row, local_rows + 2)
    own_rows = near_ids[1 : local_rows + 1]
    row_mask = jnp.stack(
        [near_ids[row_tap : row_tap + local_rows] == own_rows for row_tap in range(3)], axis=1
    ).astype(jnp.bfloat16)
    key_ids = jnp.repeat(row_ids, canvas_cols)
    query_ids = jnp.repeat(own_rows, canvas_cols)
    grid_shape = (local_rows, canvas_cols, channels)
    inputs = features[0].reshape(pixels, channels).astype(jnp.float32)
    normed_one, inverse_one, pre_one = norm_forward(inputs, norm_gains[0], norm_shifts[0], members)
    act_one = swish(pre_one).astype(jnp.bfloat16).reshape(grid_shape)
    middle, taps_one = conv_forward(act_one, row_mask, conv_weights[0], conv_biases[0])
    normed_two, inverse_two, pre_two = norm_forward(middle, norm_gains[1], norm_shifts[1], members)
    act_two = swish(pre_two).astype(jnp.bfloat16).reshape(grid_shape)
    branch, taps_two = conv_forward(act_two, row_mask, conv_weights[1], conv_biases[1])
    residual = inputs + branch
    normed_three, inverse_three, pre_three = norm_forward(
        residual, norm_gains[2], norm_shifts[2], members
    )
    attn_input = pre_three.astype(jnp.bfloat16)
    mixed = jnp.dot(attn_input, qkv_weight, preferred_element_type=jnp.float32)
    queries = (mixed[:, :channels] + qv_bias[0]).astype(jnp.bfloat16)
    key_rows = mixed[:, channels : 2 * channels].astype(jnp.bfloat16)
    value_rows = (mixed[:, 2 * channels :] + qv_bias[1]).astype(jnp.bfloat16)
    running_max = jnp.full((pixels,), masked_score, jnp.float32)
    key_piece = lax.all_gather(key_rows, "height", axis=0, tiled=True)
    value_piece = lax.all_gather(value_rows, "height", axis=0, tiled=True)
    scores = (
        lax.dot_general(
            queries, key_piece, (((1,), (1,)), ((), ())), preferred_element_type=jnp.float32
        )
        * score_scale
    )
    same_tile = query_ids[:, None] == key_ids[None, :]
    scores = jnp.where(same_tile, scores, masked_score)
    new_max = jnp.maximum(running_max, jnp.max(scores, axis=1))
    weights = jnp.where(same_tile, jnp.exp(scores - new_max[:, None]), 0.0)
    summed_out = jnp.dot(
        weights.astype(jnp.bfloat16), value_piece, preferred_element_type=jnp.float32
    )
    total_weight = jnp.sum(weights, axis=1)
    log_total = new_max + jnp.log(total_weight)
    attended = summed_out / total_weight[:, None]
    attended_low = attended.astype(jnp.bfloat16)
    output = (
        residual
        + jnp.dot(attended_low, proj_weight, preferred_element_type=jnp.float32)
        + proj_bias
    )
    out_grad = cotangent[0].reshape(pixels, channels)
    out_grad_full = out_grad.astype(jnp.float32)
    proj_grad = lax.dot_general(
        attended_low, out_grad, (((0,), (0,)), ((), ())), preferred_element_type=jnp.float32
    )
    proj_bias_grad = jnp.sum(out_grad_full, axis=0)
    attended_grad = lax.dot_general(
        out_grad, proj_weight, (((1,), (1,)), ((), ())), preferred_element_type=jnp.float32
    ).astype(jnp.bfloat16)
    row_dots = jnp.sum(attended_grad.astype(jnp.float32) * attended, axis=1)
    block_rows = pixels * min(height_size, 8)
    zero_block = jnp.zeros((pixels, channels), jnp.float32)
    key_all, value_all = (
        lax.all_gather(key_rows, "height", axis=0, tiled=True),
        lax.all_gather(value_rows, "height", axis=0, tiled=True),
    )
    query_all, grad_all = (
        lax.all_gather(queries, "height", axis=0, tiled=True),
        lax.all_gather(attended_grad, "height", axis=0, tiled=True),
    )
    total_all, dots_all = (
        lax.all_gather(log_total, "height", axis=0, tiled=True),
        lax.all_gather(row_dots, "height", axis=0, tiled=True),
    )

    def own_query_step(running, block_index):
        offset = block_index * block_rows
        key_part = take_rows(key_all, offset, block_rows)
        rounded, score_grad = score_grads(
            queries,
            attended_grad,
            log_total,
            row_dots,
            query_ids,
            key_part,
            take_rows(value_all, offset, block_rows),
            take_rows(key_ids, offset, block_rows),
            score_scale,
        )
        return (
            running
            + jnp.dot(score_grad, key_part, preferred_element_type=jnp.float32) * score_scale,
            None,
        )

    def own_key_step(running, block_index):
        offset = block_index * block_rows
        query_part = take_rows(query_all, offset, block_rows)
        grad_part = take_rows(grad_all, offset, block_rows)
        rounded, score_grad = score_grads(
            query_part,
            grad_part,
            take_rows(total_all, offset, block_rows),
            take_rows(dots_all, offset, block_rows),
            take_rows(key_ids, offset, block_rows),
            key_rows,
            value_rows,
            query_ids,
            score_scale,
        )
        key_part = (
            lax.dot_general(
                score_grad, query_part, (((0,), (0,)), ((), ())), preferred_element_type=jnp.float32
            )
            * score_scale
        )
        value_part = lax.dot_general(
            rounded, grad_part, (((0,), (0,)), ((), ())), preferred_element_type=jnp.float32
        )
        return ((running[0] + key_part, running[1] + value_part), None)

    block_count = key_all.shape[0] // block_rows
    query_grad, unused_one = lax.scan(own_query_step, zero_block, jnp.arange(block_count))
    (key_grad, value_grad), unused_two = lax.scan(
        own_key_step, (zero_block, zero_block), jnp.arange(block_count)
    )
    query_low = query_grad.astype(jnp.bfloat16)
    key_low = key_grad.astype(jnp.bfloat16)
    value_low = value_grad.astype(jnp.bfloat16)
    stacked_grad = jnp.concatenate([query_low, key_low, value_low], axis=1)
    qkv_grad = lax.dot_general(
        attn_input, stacked_grad, (((0,), (0,)), ((), ())), preferred_element_type=jnp.float32
    )
    qv_grad = jnp.stack(
        [
            jnp.sum(query_low.astype(jnp.float32), axis=0),
            jnp.sum(value_low.astype(jnp.float32), axis=0),
        ]
    )
    normed_grad = lax.dot_general(
        stacked_grad, qkv_weight, (((1,), (1,)), ((), ())), preferred_element_type=jnp.float32
    )
    back_three, gain_three, shift_three = norm_backward(
        normed_grad, normed_three, inverse_three, norm_gains[2], members
    )
    residual_grad = out_grad_full + back_three
    grad_two = residual_grad.astype(jnp.bfloat16).reshape(grid_shape)
    act_two_grad, weight_two_grad, bias_two_grad = conv_backward(
        grad_two, row_mask, conv_weights[1], taps_two
    )
    middle_grad, gain_two, shift_two = norm_backward(
        act_two_grad * swish_slope(pre_two), normed_two, inverse_two, norm_gains[1], members
    )
    grad_one = middle_grad.astype(jnp.bfloat16).reshape(grid_shape)
    act_one_grad, weight_one_grad, bias_one_grad = conv_backward(
        grad_one, row_mask, conv_weights[0], taps_one
    )
    input_back, gain_one, shift_one = norm_backward(
        act_one_grad * swish_slope(pre_one), normed_one, inverse_one, norm_gains[0], members
    )
    input_grad = residual_grad + input_back
    conv_grad = jnp.stack([weight_one_grad, weight_two_grad])
    conv_part = lax.psum_scatter(conv_grad, "height", scatter_dimension=4, tiled=True)
    conv_part = lax.psum_scatter(
        conv_part.astype(jnp.bfloat16), "canvas", scatter_dimension=3, tiled=True
    ).astype(jnp.float32)
    summed = lax.psum(
        (
            jnp.stack([gain_one, gain_two, gain_three]),
            jnp.stack([shift_one, shift_two, shift_three]),
            jnp.stack([bias_one_grad, bias_two_grad]),
            qkv_grad,
            qv_grad,
            proj_grad,
            proj_bias_grad,
        ),
        ("canvas", "height"),
    )
    return (
        output.astype(jnp.bfloat16).reshape((1,) + grid_shape),
        input_grad.astype(jnp.bfloat16).reshape((1,) + grid_shape),
        summed[0],
        summed[1],
        conv_part,
        summed[2],
        summed[3],
        summed[4],
        summed[5],
        summed[6],
    )


def fold(block):
    rows, width = block.shape
    return jnp.sum(block.reshape(rows // 8, 8, width), axis=0)


def group_lanes(block, group):
    lane = lax.broadcasted_iota(jnp.int32, block.shape, 1)
    width = block.shape[1]
    step = 1
    while step < group:
        above = pltpu.roll(block, step, 1)
        below = pltpu.roll(block, width - step, 1)
        block = block + jnp.where((lane & step) != 0, above, below)
        step *= 2
    return block


def group_mean(partial, members):
    spread = group_lanes(partial, partial.shape[1] // GROUPS)
    return jnp.sum(spread, axis=0, keepdims=True) * (1.0 / members)


def widen(block, width):
    return jnp.concatenate([block] * (width // block.shape[1]), axis=1)


def each_block(pixels, block, body, carry=0):
    def step(index, carry):
        return body(pl.ds(pl.multiple_of(index * block, block), block), carry)

    return lax.fori_loop(0, pixels // block, step, carry)


def each_chunk(pixels, body, carry):
    return each_block(pixels, CHUNK, body, carry)


def aligned(start, step):
    return start if isinstance(start, int) else pl.multiple_of(start, step)


class RunningStats:
    def __init__(self, channels):
        self.width = channels // GROUPS
        self.reference = None
        self.sums = self.squares = jnp.zeros((8, channels), jnp.float32)

    def add(self, block):
        if self.reference is None:
            self.reference = group_mean(block[0:8], 8.0 * self.width)
        offset = block - self.reference
        self.sums = self.sums + fold(offset)
        self.squares = self.squares + fold(offset * offset)

    def finish(self, pixels):
        both = group_lanes(jnp.concatenate([self.sums, self.squares], axis=0), self.width)
        share = 1.0 / (pixels * self.width)
        offset = column_total(both[0:8]) * share
        variance = column_total(both[8:16]) * share - offset * offset
        return self.reference + offset, lax.rsqrt(jnp.maximum(variance, 0.0) + epsilon)


def put_taps(taps_ref, block, rows, cols):
    count, channels = block.shape
    place = lax.broadcasted_iota(jnp.int32, block.shape, 0) & (cols - 1)
    left = jnp.where(place == 0, 0.0, pltpu.roll(block, 1, 0))
    right = jnp.where(place == cols - 1, 0.0, pltpu.roll(block, count - 1, 0))
    inner = pl.ds(aligned(rows.start + cols, cols), count)
    taps_ref[inner, 0:channels] = left.astype(jnp.bfloat16)
    taps_ref[inner, channels : 2 * channels] = block.astype(jnp.bfloat16)
    taps_ref[inner, 2 * channels :] = right.astype(jnp.bfloat16)


def clear_edges(taps_ref, cols):
    edge = jnp.zeros((cols, taps_ref.shape[1]), taps_ref.dtype)
    taps_ref[0:cols, :] = edge
    taps_ref[taps_ref.shape[0] - cols :, :] = edge


def begin_conv(taps_ref, product, total_ref, fill, first, cols):
    for start in range(0, total_ref.shape[0], FILL_ROWS):
        for inner in range(start, start + FILL_ROWS, CHUNK):
            fill(pl.ds(inner, CHUNK))
        rows = pl.ds(start, FILL_ROWS)
        total_ref[rows, :] = first(rows, product(taps_ref, pl.ds(start + cols, FILL_ROWS), 1))


def add_rows(taps_ref, product, mask_ref, total_ref, stop, cols):
    rows = pl.ds(0, stop)
    part = product(taps_ref, rows, 0)
    total_ref[rows, :] += widen(mask_ref[0, rows, :], total_ref.shape[1]) * part


def end_conv(taps_ref, product, mask_ref, total_ref, last, cols, old_ref=None, pending=None):
    pixels, channels = total_ref.shape
    old_ref = total_ref if old_ref is None else old_ref
    pending = pixels if pending is None else pending
    for start in range(0, pixels, FILL_ROWS):
        rows = pl.ds(start, FILL_ROWS)
        value = old_ref[rows, :]
        for row_tap in (0, 2) if start >= pending else (2,):
            part = product(taps_ref, pl.ds(start + row_tap * cols, FILL_ROWS), row_tap)
            value = value + widen(mask_ref[row_tap // 2, rows, :], channels) * part
        total_ref[rows, :] = last(rows, value)


def run_conv(taps_ref, product, mask_ref, total_ref, fill, first, last, cols):
    begin_conv(taps_ref, product, total_ref, fill, first, cols)
    add_rows(taps_ref, product, mask_ref, total_ref, total_ref.shape[0], cols)
    end_conv(taps_ref, product, mask_ref, total_ref, last, cols)


def product_forward(weight_ref):
    channels = weight_ref.shape[-1]

    def product(taps_ref, shifted, row_tap):
        return jnp.dot(
            taps_ref[shifted, :],
            weight_ref[row_tap].reshape(3 * channels, channels),
            preferred_element_type=jnp.float32,
        )

    return product


def product_backward(weight_ref):
    def product(taps_ref, shifted, row_tap):
        return lax.dot_general(
            taps_ref[shifted, :],
            weight_ref[row_tap],
            (((1,), (1,)), ((), ())),
            preferred_element_type=jnp.float32,
        )

    return product


def activation(read, mean, inverse, gain, shift, act_ref, taps_ref, cols):
    scale, offset = 0.5 * inverse * gain, 0.5 * shift

    def fill(rows):
        half = (read(rows) - mean) * scale + offset
        act = half * (1.0 + jnp.tanh(half))
        act_ref[rows, :] = act.astype(jnp.bfloat16)
        put_taps(taps_ref, act, rows, cols)

    return fill


def back_means(sums, gain, pixels):
    channels = gain.shape[1]
    members = float(pixels * (channels // GROUPS))
    return group_mean(sums[0] * gain, members), group_mean(sums[1] * gain, members)


def column_total(partial):
    return jnp.sum(partial, axis=0, keepdims=True)


def weight_part(act_ref, narrow, lanes_ref, flip_ref, columns_ref, part_ref, cols):
    pixels, channels = act_ref.shape
    height = lax.axis_index("height")
    share = NARROW // 2
    flip_ref[...] = narrow.T
    own = pl.ds(pl.multiple_of((height % 2) * share, share), share)
    grad = flip_ref[own, :].astype(jnp.float32)
    column = lax.broadcasted_iota(jnp.int32, grad.shape, 1) & (cols - 1)
    for col_tap in range(3):
        shifted = grad
        if col_tap == 0:
            shifted = jnp.where(column == cols - 1, 0.0, pltpu.roll(grad, pixels - 1, 1))
        elif col_tap == 2:
            shifted = jnp.where(column == 0, 0.0, pltpu.roll(grad, 1, 1))
        for row_tap in range(3):
            tap = 3 * row_tap + col_tap
            place = slice(tap * share, (tap + 1) * share)
            if row_tap == 1:
                columns_ref[place, :] = shifted.astype(jnp.bfloat16)
                continue
            side, turn = (0, pixels - cols) if row_tap == 0 else (1, cols)
            masked = (shifted * lanes_ref[side : side + 1, :]).astype(jnp.bfloat16)
            columns_ref[place, :] = pltpu.roll(masked, turn, 1)
    part_ref[...] = jnp.dot(
        columns_ref[...], act_ref[...], preferred_element_type=jnp.float32
    ).astype(jnp.bfloat16)


def begin_back(read, weights_ref, mask_ref, taps_ref, total_ref, stop, cols):
    clear_edges(taps_ref, cols)

    def fill(rows):
        put_taps(taps_ref, read(rows), rows, cols)

    product = product_backward(weights_ref)
    begin_conv(taps_ref, product, total_ref, fill, lambda rows, part: part, cols)
    if stop:
        add_rows(taps_ref, product, mask_ref, total_ref, stop, cols)


def finish_back(
    weights_ref,
    mask_ref,
    taps_ref,
    total_ref,
    read,
    table_ref,
    which,
    cols,
    old_ref=None,
    pending=None,
):
    mean, inverse, gain, shift = norm_rows(table_ref, which)
    scale, offset = 0.5 * inverse * gain, 0.5 * shift
    sums = []

    def slope(rows, value):
        centered = read(rows) - mean
        half = centered * scale + offset
        turn = jnp.tanh(half)
        double = value * ((1.0 + turn) * (1.0 + half * (1.0 - turn)))
        sums.append((fold(double), fold(double * centered)))
        return double

    product = product_backward(weights_ref)
    end_conv(taps_ref, product, mask_ref, total_ref, slope, cols, old_ref, pending)
    plain, cross = sum(pair[0] for pair in sums), sum(pair[1] for pair in sums)
    return 0.5 * plain, 0.5 * inverse * cross


def norm_back(total_ref, double, sums, read, table_ref, which, pixels, scales_ref=None):
    mean, inverse, gain, shift = norm_rows(table_ref, which)
    mean_grad, mean_cross = back_means(sums, gain, pixels)
    slope = inverse * gain * (0.5 if double else 1.0)
    level, tilt = inverse * mean_grad, inverse * inverse * mean_cross
    if scales_ref is not None:
        for row, scales in enumerate((mean, slope, level, tilt)):
            scales_ref[row : row + 1, :] = scales

    def back(rows, inner):
        return total_ref[inner, :] * slope - level - (read(rows) - mean) * tilt

    return back


def own_lanes():
    block = lax.axis_index("height") // 2
    return pl.ds(pl.multiple_of(block * NARROW, NARROW), NARROW)


def narrow_back(total_ref, value_ref, scales_ref):
    lanes = own_lanes()
    mean, slope, level, tilt = (scales_ref[row : row + 1, lanes] for row in range(4))
    return total_ref[:, lanes] * slope - level - (value_ref[:, lanes] - mean) * tilt


def turn_kernel(grad_ref, mask_ref, weights_ref, total_ref, taps_ref, *, cols):
    def read(rows):
        return grad_ref[rows, :].astype(jnp.float32)

    begin_back(read, weights_ref.at[1], mask_ref, taps_ref, total_ref, EARLY_ROWS, cols)


def norm_rows(table_ref, which):
    picks = (2 * which, 2 * which + 1, 6 + which, 9 + which)
    return tuple(table_ref[pick : pick + 1, :] for pick in picks)


def build_masks(ids_ref, mask_ref, lanes_ref, id_rows_ref, id_cols_ref, cols):
    rows = ids_ref.shape[1]

    def one_row(row, carry):
        here = ids_ref[0, row]
        place = pl.ds(pl.multiple_of(row * cols, cols), cols)
        id_rows_ref[place, :] = jnp.full((cols, LANES), here, jnp.int32)
        for side, other in ((0, row - 1), (1, row + 1)):
            inside = jnp.logical_and(other >= 0, other < rows)
            other_id = ids_ref[0, jnp.clip(other, 0, rows - 1)]
            same = jnp.where(jnp.logical_and(inside, other_id == here), 1.0, 0.0)
            mask_ref[side, place, :] = jnp.full((cols, LANES), same, jnp.float32)
        return carry

    lax.fori_loop(0, rows, one_row, 0)
    lane = lax.broadcasted_iota(jnp.int32, (8, LANES), 1)
    each = LANES // cols
    for block in range(rows // each):
        ids = jnp.full((8, LANES), ids_ref[0, block * each], jnp.int32)
        for step in range(1, each):
            ids = jnp.where(lane >= step * cols, ids_ref[0, block * each + step], ids)
        id_cols_ref[:, block * LANES : (block + 1) * LANES] = ids
    ids = id_cols_ref[...].astype(jnp.float32)
    pixels = ids.shape[1]
    pixel = lax.broadcasted_iota(jnp.int32, ids.shape, 1)
    above = jnp.where(pixel < cols, -1.0, pltpu.roll(ids, cols, 1))
    below = jnp.where(pixel >= pixels - cols, -1.0, pltpu.roll(ids, pixels - cols, 1))
    lanes_ref[0:1, :] = jnp.where(above == ids, 1.0, 0.0)[0:1]
    lanes_ref[1:2, :] = jnp.where(below == ids, 1.0, 0.0)[0:1]


def place_pieces(pieces, whole_ref, sems):
    own_pixels = whole_ref.shape[0] // len(pieces)
    height = lax.axis_index("height")
    copies = []
    for place, piece in enumerate(pieces):
        piece = piece.at[piece.shape[0] - own_pixels : piece.shape[0], :]
        start = pl.multiple_of((height ^ place) * own_pixels, own_pixels)
        rows = pl.ds(start, own_pixels)
        copies.append(pltpu.make_async_copy(piece, whole_ref.at[rows, :], sems.at[place]))
    return copies


def hold_kernel(
    ids_hbm,
    gains_hbm,
    shifts_hbm,
    biases_hbm,
    weights_hbm,
    qkv_hbm,
    proj_hbm,
    qv_bias_hbm,
    proj_bias_hbm,
    weights_ref,
    turned_ref,
    qkv_ref,
    proj_ref,
    table_ref,
    mask_ref,
    lanes_ref,
    id_rows_ref,
    id_cols_ref,
    ids_ref,
    gains_ref,
    shifts_ref,
    biases_ref,
    qv_bias_ref,
    proj_bias_ref,
    sems,
    *,
    cols,
):
    channels = weights_ref.shape[-1]
    small = [
        (ids_hbm, ids_ref),
        (gains_hbm, gains_ref),
        (shifts_hbm, shifts_ref),
        (biases_hbm, biases_ref),
        (qv_bias_hbm, qv_bias_ref),
        (proj_bias_hbm, proj_bias_ref),
    ]
    large = [(weights_hbm, weights_ref), (qkv_hbm, qkv_ref), (proj_hbm, proj_ref)]
    for which in range(2):
        for row_tap in range(3):
            for col_tap in range(3):
                place = slice(col_tap * channels, (col_tap + 1) * channels)
                large.append(
                    (
                        weights_hbm.at[which, 2 - row_tap, 2 - col_tap],
                        turned_ref.at[which, row_tap, :, place],
                    )
                )
    copies = [
        pltpu.make_async_copy(source, target, sems.at[index])
        for index, (source, target) in enumerate(small + large)
    ]
    for copy in copies:
        copy.start()
    for copy in copies[: len(small)]:
        copy.wait()
    build_masks(ids_ref, mask_ref, lanes_ref, id_rows_ref, id_cols_ref, cols)
    table_ref[6:9, :] = gains_ref[...]
    table_ref[9:12, :] = shifts_ref[...]
    table_ref[12:14, :] = biases_ref[...]
    table_ref[14:16, :] = qv_bias_ref[...]
    table_ref[16:17, :] = proj_bias_ref[...]
    for copy in copies[len(small) :]:
        copy.wait()


def conv_kernel(*refs, cols, count):
    pieces, refs = refs[:count], refs[count:]
    (
        weights_ref,
        params_ref,
        mask_ref,
        features_ref,
        act_one_ref,
        middle_ref,
        act_two_ref,
        residual_ref,
        table_ref,
        own_ref,
        taps_ref,
        sem,
    ) = refs
    pixels, channels = features_ref.shape
    wide = jnp.float32
    own_copy = pltpu.make_async_copy(pieces[0], own_ref, sem)
    own_copy.start()
    table_ref[...] = params_ref[...]
    clear_edges(taps_ref, cols)

    def read_input(rows):
        return features_ref[rows, :].astype(wide)

    def read_middle(rows):
        return middle_ref[rows, :]

    height = lax.axis_index("height")
    own_pixels = pixels // count
    seen = RunningStats(channels)
    for place in list(range(1, count)) + [0]:
        if place == 0:
            own_copy.wait()
        piece = (pieces[place] if place else own_ref)[0:own_pixels, :]
        start = pl.multiple_of((height ^ place) * own_pixels, own_pixels)
        features_ref[pl.ds(start, own_pixels), :] = piece
        seen.add(piece.astype(wide))
    table_ref[0:1, :], table_ref[1:2, :] = seen.finish(pixels)
    seen = RunningStats(channels)

    def keep(rows, value):
        seen.add(value)
        return value

    run_conv(
        taps_ref,
        product_forward(weights_ref.at[0]),
        mask_ref,
        middle_ref,
        activation(read_input, *norm_rows(table_ref, 0), act_one_ref, taps_ref, cols),
        lambda rows, part: part + table_ref[12:13, :],
        keep,
        cols,
    )
    table_ref[2:3, :], table_ref[3:4, :] = seen.finish(pixels)
    seen = RunningStats(channels)
    run_conv(
        taps_ref,
        product_forward(weights_ref.at[1]),
        mask_ref,
        residual_ref,
        activation(read_middle, *norm_rows(table_ref, 1), act_two_ref, taps_ref, cols),
        lambda rows, part: part + (read_input(rows) + table_ref[13:14, :]),
        keep,
        cols,
    )
    table_ref[4:5, :], table_ref[5:6, :] = seen.finish(pixels)


def score_kernel(
    qkv_ref,
    proj_ref,
    residual_ref,
    table_ref,
    id_rows_ref,
    id_cols_ref,
    normed_ref,
    query_ref,
    key_ref,
    value_ref,
    soft_ref,
    out_flip_ref,
    output_ref,
    value_flip_ref,
    *scores_refs,
    score_scale,
):
    pixels, channels = residual_ref.shape
    own_pixels = output_ref.shape[0]
    wide = jnp.float32
    exponent = score_scale * 1.4426950408889634
    mean, inverse, gain, shift = norm_rows(table_ref, 2)
    scale = inverse * gain

    def normalise(start):
        rows = slice(start, start + KEY_ROWS)
        normed = (residual_ref[rows, :] - mean) * scale + shift
        normed_ref[rows, :] = normed.astype(jnp.bfloat16)

    def project(start):
        rows = slice(start, start + KEY_ROWS)
        normed = normed_ref[rows, :]
        query_ref[rows, :] = (
            jnp.dot(normed, qkv_ref[:, 0:channels], preferred_element_type=wide)
            + table_ref[14:15, :]
        ).astype(jnp.bfloat16)
        key_ref[rows, :] = jnp.dot(
            normed, qkv_ref[:, channels : 2 * channels], preferred_element_type=wide
        ).astype(jnp.bfloat16)
        values = (
            jnp.dot(normed, qkv_ref[:, 2 * channels :], preferred_element_type=wide)
            + table_ref[15:16, :]
        ).astype(jnp.bfloat16)
        value_ref[rows, :] = values
        value_flip_ref[:, rows] = values.T

    normalise(0)
    for start in range(0, pixels, KEY_ROWS):
        if start + KEY_ROWS < pixels:
            normalise(start + KEY_ROWS)
        project(start)
    block = scores_refs[0].shape[1]
    steps = range(0, pixels, KEY_ROWS)

    def score(index):
        rows = slice(index * block, (index + 1) * block)
        for start in steps:
            keys = slice(start, start + KEY_ROWS)
            scores = lax.dot_general(
                key_ref[keys, :],
                query_ref[rows, :],
                (((1,), (1,)), ((), ())),
                preferred_element_type=wide,
            )
            same = widen(id_rows_ref[keys, :], block) == id_cols_ref[0:1, rows]
            scores_refs[index][keys, :] = jnp.where(same, scores, masked_score)

    def soften(index):
        rows = slice(index * block, (index + 1) * block)
        scores_ref = scores_refs[index]
        peak = jnp.full((8, block), masked_score, wide)
        for start in steps:
            scores = scores_ref[start : start + KEY_ROWS, :]
            peak = jnp.maximum(peak, jnp.max(scores.reshape(-1, 8, block), axis=0))
        peak = jnp.max(peak, axis=0, keepdims=True)
        total = jnp.zeros((8, block), wide)
        for start in steps:
            keys = slice(start, start + KEY_ROWS)
            powers = jnp.exp2((scores_ref[keys, :] - peak) * exponent)
            scores_ref[keys, :] = powers
            total = total + fold(powers)
        share = 1.0 / column_total(total)
        for start in steps:
            keys = slice(start, start + KEY_ROWS)
            soft_ref[keys, rows] = (scores_ref[keys, :] * share).astype(jnp.bfloat16)

    score(0)
    for index in range(len(scores_refs)):
        if index + 1 < len(scores_refs):
            score(index + 1)
        soften(index)
        rows = slice(index * block, (index + 1) * block)
        out_flip_ref[:, rows] = jnp.dot(
            value_flip_ref[...], soft_ref[:, rows], preferred_element_type=wide
        ).astype(jnp.bfloat16)
    height = lax.axis_index("height")
    own = pl.ds(pl.multiple_of(height * own_pixels, own_pixels), own_pixels)
    output_ref[...] = (
        residual_ref[own, :]
        + lax.dot_general(
            out_flip_ref[:, own],
            proj_ref[...],
            (((0,), (0,)), ((), ())),
            preferred_element_type=wide,
        )
        + table_ref[16:17, :]
    ).astype(jnp.bfloat16)


def own_quarter():
    height = lax.axis_index("height")
    return (height & 1) * 2 + ((height >> 1) & 1)


def attention_kernel(
    proj_ref,
    normed_ref,
    query_ref,
    key_ref,
    value_ref,
    soft_ref,
    out_flip_ref,
    *refs,
    score_scale,
    count,
):
    pieces, (grad_ref, packed_ref, sums_ref), refs = (
        refs[:count],
        refs[count : count + 3],
        refs[count + 3 :],
    )
    pixels, channels = normed_ref.shape
    blocks = pixels // SCORE_ROWS
    grads_refs, refs = refs[-blocks:], refs[:-blocks]
    *mixed_refs, mixed_ref, key_flip_ref, back_ref, score_grad_ref, flip_ref, sems = refs
    wide = jnp.float32
    copies = place_pieces(pieces, grad_ref, sems)
    for copy in copies:
        copy.start()
    quarter = channels // 4
    own = pl.ds(pl.multiple_of(own_quarter() * quarter, quarter), quarter)
    flip_ref[...] = normed_ref[:, own].T
    key_flip_ref[...] = key_ref[...].T
    for copy in copies:
        copy.wait()
    block, count = SCORE_ROWS, blocks
    steps = range(0, pixels, KEY_ROWS)

    def block_rows(index):
        return slice(index * block, (index + 1) * block)

    for index in range(count):
        back_ref[block_rows(index), :] = lax.dot_general(
            grad_ref[block_rows(index), :],
            proj_ref[...],
            (((1,), (1,)), ((), ())),
            preferred_element_type=wide,
        ).astype(jnp.bfloat16)

    def weigh(index):
        total = jnp.zeros((8, block), wide)
        for start in steps:
            keys = slice(start, start + KEY_ROWS)
            weight_grad = lax.dot_general(
                value_ref[keys, :],
                back_ref[block_rows(index), :],
                (((1,), (1,)), ((), ())),
                preferred_element_type=wide,
            )
            grads_refs[index][keys, :] = weight_grad
            total = total + fold(soft_ref[keys, block_rows(index)].astype(wide) * weight_grad)
        return column_total(total)

    def slope(index, dots):
        for start in steps:
            keys = slice(start, start + KEY_ROWS)
            weights = soft_ref[keys, block_rows(index)].astype(wide)
            score_grad_ref[keys, block_rows(index)] = (
                weights * (grads_refs[index][keys, :] - dots)
            ).astype(jnp.bfloat16)

    dots = weigh(0)
    for index in range(count):
        now, rows = dots, block_rows(index)
        if index + 1 < count:
            dots = weigh(index + 1)
        slope(index, now)
        packed_ref[rows, 2 * channels :] = jnp.dot(
            soft_ref[rows, :], back_ref[...], preferred_element_type=wide
        ).astype(jnp.bfloat16)
        query_grad = jnp.dot(
            key_flip_ref[...], score_grad_ref[:, rows], preferred_element_type=wide
        )
        packed_ref[rows, 0:channels] = (query_grad * score_scale).astype(jnp.bfloat16).T
    for index in range(count):
        rows = block_rows(index)
        packed_ref[rows, channels : 2 * channels] = (
            jnp.dot(score_grad_ref[rows, :], query_ref[...], preferred_element_type=wide)
            * score_scale
        ).astype(jnp.bfloat16)

    def pack(rows, carry):
        return (
            carry[0] + fold(packed_ref[rows, 0:channels].astype(wide)),
            carry[1] + fold(packed_ref[rows, 2 * channels :].astype(wide)),
            carry[2] + fold(grad_ref[rows, :].astype(wide)),
        )

    zeros = jnp.zeros((8, channels), wide)
    totals = zeros, zeros, zeros
    for start in range(0, pixels, CHUNK):
        totals = pack(pl.ds(start, CHUNK), totals)
    sums_ref[...] = jnp.zeros(sums_ref.shape, wide)
    for row, total in enumerate(totals):
        sums_ref[8 + row : 9 + row, :] = column_total(total)
    mixed_ref[:, 0 : 3 * channels] = jnp.dot(
        flip_ref[...], packed_ref[...], preferred_element_type=wide
    ).astype(jnp.bfloat16)
    mixed_ref[:, 3 * channels :] = jnp.dot(
        out_flip_ref[own, :], grad_ref[...], preferred_element_type=wide
    ).astype(jnp.bfloat16)
    share = quarter // len(mixed_refs)
    me = lax.axis_index("canvas")
    for step, target in enumerate(mixed_refs):
        target[...] = mixed_ref[pl.ds(pl.multiple_of((me ^ step) * share, share), share), :]


def third_kernel(
    qkv_ref,
    grad_ref,
    packed_ref,
    residual_ref,
    table_ref,
    act_two_ref,
    lanes_ref,
    old_sums_ref,
    residual_grad_ref,
    grad_two_ref,
    sums_ref,
    part_ref,
    total_ref,
    flip_ref,
    columns_ref,
    *,
    cols,
):
    pixels, channels = residual_ref.shape
    block = FILL_ROWS
    wide = jnp.float32
    mean, inverse, gain, shift = norm_rows(table_ref, 2)
    zeros = jnp.zeros((8, channels), wide)

    sums = (zeros, zeros)
    for start in range(0, pixels, block):
        rows = pl.ds(start, block)
        normed_grad = lax.dot_general(
            packed_ref[rows, :], qkv_ref[...], (((1,), (1,)), ((), ())), preferred_element_type=wide
        )
        total_ref[rows, :] = normed_grad
        centered = residual_ref[rows, :] - mean
        sums = sums[0] + fold(normed_grad), sums[1] + fold(normed_grad * centered)
    sums = sums[0], sums[1] * inverse
    sums_ref[...] = old_sums_ref[...]
    sums_ref[5:6, :] = column_total(sums[1])
    sums_ref[6:7, :] = column_total(sums[0])
    back = norm_back(
        total_ref, False, sums, lambda rows: residual_ref[rows, :], table_ref, 2, pixels
    )

    def finish(rows, carry):
        total = grad_ref[rows, :].astype(wide) + back(rows, rows)
        residual_grad_ref[rows, :] = total
        low = total.astype(jnp.bfloat16)
        grad_two_ref[rows, :] = low
        return carry + fold(low.astype(wide))

    sums_ref[7:8, :] = column_total(each_chunk(pixels, finish, zeros))
    narrow = grad_two_ref[:, own_lanes()]
    weight_part(act_two_ref, narrow, lanes_ref, flip_ref, columns_ref, part_ref, cols)


def second_kernel(
    old_total_ref,
    taps_ref,
    middle_ref,
    table_ref,
    act_one_ref,
    mask_ref,
    lanes_ref,
    weights_ref,
    old_sums_ref,
    part_two_ref,
    total_ref,
    scales_ref,
    sums_ref,
    keep_one_ref,
    send_one_ref,
    keep_two_ref,
    send_two_ref,
    flip_ref,
    columns_ref,
    part_ref,
    *,
    cols,
):
    pixels, channels = middle_ref.shape

    def read(rows):
        return middle_ref[rows, :]

    sums = finish_back(
        weights_ref.at[1],
        mask_ref,
        taps_ref,
        total_ref,
        read,
        table_ref,
        1,
        cols,
        old_total_ref,
        EARLY_ROWS,
    )
    norm_back(total_ref, True, sums, read, table_ref, 1, pixels, scales_ref)
    narrow = narrow_back(total_ref, middle_ref, scales_ref).astype(jnp.bfloat16)
    weight_part(act_one_ref, narrow, lanes_ref, flip_ref, columns_ref, part_ref, cols)
    sums_ref[...] = old_sums_ref[...]
    sums_ref[2:3, :] = column_total(sums[1])
    sums_ref[3:4, :] = column_total(sums[0])
    keep_half(part_ref, keep_one_ref, send_one_ref)
    keep_half(part_two_ref, keep_two_ref, send_two_ref)


def near_far():
    core = lax.axis_index("height") & 1
    return 1 + core, 2 - core


def keep_half(source_ref, keep_ref, send_ref):
    me = lax.axis_index("canvas")
    near, far = near_far()
    rows, width = keep_ref.shape[0] // 2, keep_ref.shape[1]
    for target_ref, flip in ((keep_ref, 0), (send_ref, near)):
        for slot, other in enumerate((0, far)):
            place = pl.ds(pl.multiple_of((me ^ flip ^ other) * width, width), width)
            target_ref[slot * rows : (slot + 1) * rows, :] = source_ref[:, place]


def first_kernel(
    total_two_ref,
    scales_ref,
    middle_ref,
    features_ref,
    table_ref,
    mask_ref,
    old_sums_ref,
    weights_ref,
    own_ref,
    sums_ref,
    partial_ref,
    total_ref,
    taps_ref,
    *,
    cols,
):
    def read(rows):
        return features_ref[rows, :].astype(jnp.float32)

    mean, slope, level, tilt = (scales_ref[row : row + 1, :] for row in range(4))
    grad_sums = []

    def read_grad(rows):
        grad = total_two_ref[rows, :] * slope - level - (middle_ref[rows, :] - mean) * tilt
        grad = grad.astype(jnp.bfloat16).astype(jnp.float32)
        grad_sums.append(fold(grad))
        return grad

    weights = weights_ref.at[0]
    begin_back(read_grad, weights, mask_ref, taps_ref, total_ref, total_ref.shape[0], cols)
    sums = finish_back(weights, mask_ref, taps_ref, total_ref, read, table_ref, 0, cols)
    partial_ref[0:8, :], partial_ref[8:16, :] = sums
    sums_ref[...] = old_sums_ref[...]
    sums_ref[0:1, :] = column_total(sums[1])
    sums_ref[1:2, :] = column_total(sums[0])
    sums_ref[4:5, :] = column_total(sum(grad_sums))
    count = own_ref.shape[0]
    own = pl.ds(pl.multiple_of(lax.axis_index("height") * count, count), count)
    own_ref[...] = total_ref[own, :]


def own_kernel(
    own_ref, partial_ref, features_ref, residual_grad_ref, table_ref, input_grad_ref
):
    def read(rows):
        return features_ref[rows, :].astype(jnp.float32)

    sums = partial_ref[0:8, :], partial_ref[8:16, :]
    pixels = features_ref.shape[0]
    back = norm_back(own_ref, True, sums, read, table_ref, 0, pixels)
    count = own_ref.shape[0]
    own = pl.ds(pl.multiple_of(lax.axis_index("height") * count, count), count)
    total = residual_grad_ref[own, :] + back(own, slice(0, count))
    input_grad_ref[...] = total.astype(jnp.bfloat16)


def place_kernel(*refs):
    joints, packed_ref = refs[:-1], refs[-1]
    share = packed_ref.shape[0] // len(joints)
    me = lax.axis_index("canvas")
    for step, joint in enumerate(joints):
        place = pl.ds(pl.multiple_of((me ^ step) * share, share), share)
        packed_ref[place, :] = joint[...]


def cut_kernel(packed_ref, *half_refs):
    rows = half_refs[0].shape[0]
    for index, half_ref in enumerate(half_refs):
        half_ref[...] = packed_ref[index * rows : (index + 1) * rows, :]


def spread_quarters(packed, flips, qkv_ref, proj_ref, qkv_hbm, proj_hbm, sems):
    quarter = packed[0].shape[0]
    inner = qkv_ref.shape[2]
    copies = []
    for index, packed_ref in enumerate(packed):
        owner = own_quarter() ^ flips[index]
        rows = pl.ds(pl.multiple_of(owner * quarter, quarter), quarter)
        qkv_ref[index] = packed_ref[:, 0:inner].astype(jnp.float32)
        proj_ref[index] = packed_ref[:, inner:].astype(jnp.float32)
        for which, (held, target) in enumerate(((qkv_ref, qkv_hbm), (proj_ref, proj_hbm))):
            copy = pltpu.make_async_copy(held.at[index], target.at[rows, :], sems.at[index, which])
            copy.start()
            copies.append(copy)
    return copies


def join_kernel(*refs):
    packed, (qkv_hbm, proj_hbm, qkv_ref, proj_ref, sems) = refs[:-5], refs[-5:]
    copies = spread_quarters(packed, [0, 2], qkv_ref, proj_ref, qkv_hbm, proj_hbm, sems)
    for copy in copies:
        copy.wait()


def halve_kernel(keep_ref, got_ref, hold_ref, send_ref):
    total = keep_ref[...].astype(jnp.float32) + got_ref[...].astype(jnp.float32)
    rows = hold_ref.shape[0]
    hold_ref[...] = total[0:rows]
    send_ref[0:rows, :] = total[rows:].astype(jnp.bfloat16)


def halve_both_kernel(
    keep_ref, got_ref, keep_two_ref, got_two_ref, hold_ref, send_ref, hold_two_ref
):
    rows = hold_ref.shape[0]
    halve_kernel(keep_ref, got_ref, hold_ref, send_ref)
    halve_kernel(keep_two_ref, got_two_ref, hold_two_ref, send_ref.at[rows : 2 * rows, :])


def last_kernel(
    chip_ref,
    both_a_ref,
    both_b_ref,
    old_qkv,
    old_proj,
    qkv_hbm,
    proj_hbm,
    qkv_ref,
    proj_ref,
    sems,
):
    copies = []
    rows = both_a_ref.shape[0]
    inner = qkv_ref.shape[2]
    chips = (chip_ref.at[0:rows, :], chip_ref.at[rows : 2 * rows, :])
    for index, piece_ref in enumerate((*chips, both_a_ref, both_b_ref)):
        start = ((own_quarter() ^ (1 if index < 2 else 3)) * 2 + index % 2) * rows
        target = pl.ds(pl.multiple_of(start, rows), rows)
        qkv_ref[index] = piece_ref[:, 0:inner].astype(jnp.float32)
        proj_ref[index] = piece_ref[:, inner:].astype(jnp.float32)
        for which, (held, whole) in enumerate(((qkv_ref, qkv_hbm), (proj_ref, proj_hbm))):
            copy = pltpu.make_async_copy(held.at[index], whole.at[target, :], sems.at[index, which])
            copy.start()
            copies.append(copy)
    for copy in copies:
        copy.wait()


def sums_kernel(
    sums_ref,
    got_sums_ref,
    hold_one_ref,
    hold_two_ref,
    got_ref,
    share_ref,
    gains_ref,
    shifts_ref,
    conv_ref,
    qv_ref,
    bias_ref,
):
    rows = hold_one_ref.shape[0]
    for which, hold_ref in enumerate((hold_one_ref, hold_two_ref)):
        got = got_ref[which * rows : (which + 1) * rows, :].astype(jnp.float32)
        share_ref[which] = (hold_ref[...] + got).reshape(share_ref.shape[1:])
    total = sums_ref[...] + got_sums_ref[...]
    for row, start in enumerate((0, 2, 5)):
        gains_ref[row : row + 1, :] = total[start : start + 1]
        shifts_ref[row : row + 1, :] = total[start + 1 : start + 2]
    conv_ref[0:1, :] = total[4:5]
    conv_ref[1:2, :] = total[7:8]
    qv_ref[...] = total[8:10]
    bias_ref[...] = total[10:11]


def call_kernel(kernel, outputs, scratch, operands, places, flops, limit, out_places=None, aliases={}):
    out_places = out_places or "v" * len(outputs)
    spaces = {
        "v": pl.BlockSpec(memory_space=pltpu.VMEM),
        "s": pl.BlockSpec(memory_space=pltpu.SMEM),
        "h": pl.BlockSpec(memory_space=pl.ANY),
        "o": pl.BlockSpec(memory_space=pltpu.VMEM),
        "a": pl.BlockSpec(memory_space=pl.ANY),
    }
    moved = 8 * flops // LANES
    held = {"v": pltpu.VMEM, "h": pltpu.HBM, "o": jax.ShapeDtypeStruct}
    operands = [
        pltpu.with_memory_space_constraint(array, pltpu.HBM) if place == "h" else array
        for array, place in zip(operands, places)
    ]
    return pl.pallas_call(
        kernel,
        out_shape=[held[place](*output) for output, place in zip(outputs, out_places)],
        in_specs=[spaces[place] for place in places],
        out_specs=[spaces[place] for place in out_places],
        scratch_shapes=scratch,
        input_output_aliases=aliases,
        compiler_params=pltpu.CompilerParams(vmem_limit_bytes=limit * 2**20),
        cost_estimate=pl.CostEstimate(flops=flops, bytes_accessed=moved, transcendentals=0),
    )(*operands)


def send_height(block, step):
    size = lax.axis_size("height")
    return lax.ppermute(block, "height", [(i, i ^ step) for i in range(size)])


def with_cores(blocks, other):
    pieces = [blocks[0], other]
    for block in blocks[1:]:
        pieces += [block, send_height(block, 1)]
    return pieces


def send_canvas(block, step):
    size = lax.axis_size("canvas")
    return lax.ppermute(block, "canvas", [(i, i ^ step) for i in range(size)])


def send_phase(block, phase):
    canvases, size = lax.axis_size("canvas"), lax.axis_size("height")
    pairs = []
    for canvas in range(canvases):
        for height in range(size):
            step = 2 if (height ^ phase) & 1 else 1
            pairs.append((canvas * size + height, (canvas ^ step) * size + height))
    return lax.ppermute(block, ("canvas", "height"), pairs)


def trade_canvas(pieces):
    return [pieces[0]] + [send_canvas(piece, step) for step, piece in enumerate(pieces) if step]


def whole_canvas(
    features,
    tile_ids,
    norm_gains,
    norm_shifts,
    conv_weights,
    conv_biases,
    qkv_weight,
    qv_bias,
    proj_weight,
    proj_bias,
    cotangent,
):
    height_size = lax.axis_size("height")
    canvas_size = lax.axis_size("canvas")
    local_rows, cols, channels = features.shape[1:]
    all_rows = tile_ids.shape[1]
    pixels = all_rows * cols
    own_pixels = local_rows * cols
    out_share = channels // height_size
    ci_share = channels // canvas_size
    quarter = channels // 4
    row_share = quarter // canvas_size
    low, wide = jnp.bfloat16, jnp.float32

    own_features = features.reshape(own_pixels, channels)
    own_grad = cotangent.reshape(own_pixels, channels)
    steps = range(2, height_size, 2)
    held_features = [own_features] + [send_height(own_features, step) for step in steps]
    plane = ((pixels, channels), low)
    plane_wide = ((pixels, channels), wide)
    sums_shape = ((16, channels), wide)
    mixed_shapes = [((row_share, 4 * channels), low)] * canvas_size
    taps = pltpu.VMEM((pixels + 2 * cols, 3 * channels), low)
    held_wide = pltpu.VMEM((pixels, channels), wide)
    flipped = pltpu.VMEM((channels, pixels), low)
    narrow = pltpu.VMEM((NARROW, pixels), low)
    columns = pltpu.VMEM((9 * out_share, pixels), low)
    part_held = pltpu.VMEM((9 * out_share, channels), low)
    sem = pltpu.SemaphoreType.DMA
    conv_flops = 2 * 9 * pixels * channels * channels
    dot_flops = 2 * pixels * channels * channels
    score_flops = 2 * pixels * pixels * channels
    scale = channels ** (-0.5)

    (
        held_conv,
        turned,
        held_qkv,
        held_proj,
        params,
        mask,
        lane_mask,
        id_rows,
        id_cols,
    ) = call_kernel(
        functools.partial(hold_kernel, cols=cols),
        [
            (conv_weights.shape, low),
            ((2, 3, channels, 3 * channels), low),
            (qkv_weight.shape, low),
            (proj_weight.shape, low),
            ((24, channels), wide),
            ((2, pixels, LANES), wide),
            ((8, pixels), wide),
            ((pixels, LANES), jnp.int32),
            ((8, pixels), jnp.int32),
        ],
        [
            pltpu.SMEM(tile_ids.shape, jnp.int32),
            pltpu.VMEM(norm_gains.shape, wide),
            pltpu.VMEM(norm_shifts.shape, wide),
            pltpu.VMEM(conv_biases.shape, wide),
            pltpu.VMEM(qv_bias.shape, wide),
            pltpu.VMEM((1, channels), wide),
            sem((27,)),
        ],
        [
            tile_ids,
            norm_gains,
            norm_shifts,
            conv_biases,
            conv_weights,
            qkv_weight,
            proj_weight,
            qv_bias,
            proj_bias.reshape(1, channels),
        ],
        "h" * 9,
        conv_flops,
        8,
    )
    held_features[1:] = [
        lax.optimization_barrier((params, block))[1] for block in held_features[1:]
    ]
    other_core = send_height(jnp.concatenate([own_features, own_grad], axis=0), 1)
    pieces = with_cores(held_features, other_core)
    far_grad, *pieces[4::2] = lax.optimization_barrier((own_grad, *held_features[2:]))
    held_grads = [own_grad, send_height(own_grad, 2)]
    held_grads[1], pieces[2] = lax.optimization_barrier((held_grads[1], held_features[1]))
    held_grads += [send_height(far_grad, step) for step in steps[1:]]

    all_features, act_one, middle, act_two, residual, table = call_kernel(
        functools.partial(conv_kernel, cols=cols, count=height_size),
        [plane, plane, plane_wide, plane, plane_wide, ((24, channels), wide)],
        [pltpu.VMEM((own_pixels, channels), low), taps, sem],
        [*pieces, held_conv, params, mask],
        "h" + "v" * (height_size + 2),
        2 * conv_flops,
        16,
    )
    residual, *held_grads = lax.optimization_barrier((residual, *held_grads))
    grad_pieces = with_cores(held_grads, other_core)
    normed, query, key, value, soft, out_flip, output = call_kernel(
        functools.partial(score_kernel, score_scale=scale),
        [
            plane,
            plane,
            plane,
            plane,
            ((pixels, pixels), low),
            ((channels, pixels), low),
            ((own_pixels, channels), low),
        ],
        [
            flipped,
            *[pltpu.VMEM((pixels, SCORE_ROWS), wide)] * (pixels // SCORE_ROWS),
        ],
        [
            held_qkv,
            held_proj,
            residual,
            table,
            id_rows,
            id_cols,
        ],
        "vvvvvv",
        3 * dot_flops + 2 * score_flops,
        20,
        "v" * 6 + "o",
    )
    normed, *grad_pieces = lax.optimization_barrier((normed, *grad_pieces))
    all_grad, packed, sums, *mixed = call_kernel(
        functools.partial(attention_kernel, score_scale=scale, count=height_size),
        [plane, ((pixels, 3 * channels), low), sums_shape, *mixed_shapes],
        [
            pltpu.VMEM((quarter, 4 * channels), low),
            flipped,
            pltpu.VMEM((pixels, channels), low),
            pltpu.VMEM((pixels, pixels), low),
            pltpu.VMEM((quarter, pixels), low),
            sem((height_size,)),
            *[pltpu.VMEM((pixels, SCORE_ROWS), wide)] * (pixels // SCORE_ROWS),
        ],
        [held_proj, normed, query, key, value, soft, out_flip, *grad_pieces],
        "vvvvvvvh" + "a" * (height_size - 1),
        3 * dot_flops + 4 * score_flops,
        20,
    )
    mixed = trade_canvas(mixed)
    residual_grad, grad_two, sums, part_two = call_kernel(
        functools.partial(third_kernel, cols=cols),
        [plane_wide, plane, sums_shape, ((9 * out_share, channels), low)],
        [held_wide, narrow, columns],
        [held_qkv, all_grad, packed, residual, table, act_two, lane_mask, sums],
        "vvvvvvvv",
        3 * dot_flops + conv_flops // height_size,
        16,
    )
    half_total, half_taps = call_kernel(
        functools.partial(turn_kernel, cols=cols),
        [plane_wide, (taps.shape, low)],
        [],
        [grad_two, mask, turned],
        "vvv",
        2 * conv_flops // 3,
        16,
    )
    half_total, *mixed = lax.optimization_barrier((half_total, *mixed))
    mixed_sum = mixed[0].astype(wide)
    for piece in mixed[1:]:
        mixed_sum = mixed_sum + piece.astype(wide)
    mixed_sum = mixed_sum.astype(low)
    joints = trade_canvas([mixed_sum] * canvas_size)
    halves = [((2 * 9 * out_share, ci_share), low)] * 4
    total_two, scales, sums, keep_one, send_one, keep_two, send_two = call_kernel(
        functools.partial(second_kernel, cols=cols),
        [plane_wide, ((8, channels), wide), sums_shape, *halves],
        [narrow, columns, part_held],
        [half_total, half_taps, middle, table, act_one, mask, lane_mask, turned, sums, part_two],
        "v" * 10,
        conv_flops // 2,
        20,
    )
    total_two, *joints = lax.optimization_barrier((total_two, *joints))
    (own_mixed,) = call_kernel(
        place_kernel,
        [((quarter, 4 * channels), low)],
        [],
        joints,
        "v" * canvas_size,
        1,
        12,
    )
    own_mixed, send_one, send_two = lax.optimization_barrier((own_mixed, send_one, send_two))
    chip_mixed = send_height(own_mixed, 2)
    core_mixed = send_height(own_mixed, 1)
    got_one, got_two = send_phase(send_one, 0), send_phase(send_two, 0)
    own_total, sums, partial_sums = call_kernel(
        functools.partial(first_kernel, cols=cols),
        [((own_pixels, channels), wide), sums_shape, sums_shape],
        [held_wide, taps],
        [total_two, scales, middle, all_features, table, mask, sums, turned],
        "vvvvvvvv",
        1,
        20,
    )
    got_sums, own_sums = send_phase(sums, 0), sums
    sums, core_mixed, got_one, got_two = lax.optimization_barrier(
        (sums, core_mixed, got_one, got_two)
    )
    share_rows = 9 * out_share
    hold_one, send_share, hold_two = call_kernel(
        halve_both_kernel,
        [
            ((share_rows, ci_share), wide),
            ((2 * share_rows, ci_share), low),
            ((share_rows, ci_share), wide),
        ],
        [],
        [keep_one, got_one, keep_two, got_two],
        "vvvv",
        1,
        12,
    )
    got_share = send_phase(send_share, 1)

    def widened(count, rows):
        return [
            pltpu.VMEM((count, rows, 3 * channels), wide),
            pltpu.VMEM((count, rows, channels), wide),
            sem((count, 2)),
        ]

    grad_shapes = [(qkv_weight.shape, wide), (proj_weight.shape, wide)]
    core_mixed, hold_one = lax.optimization_barrier((core_mixed, hold_one))
    qkv_grad, proj_grad = call_kernel(
        join_kernel,
        grad_shapes,
        widened(2, quarter),
        [own_mixed, core_mixed],
        "vv",
        1,
        12,
        "hh",
    )
    qkv_grad, chip_mixed, got_sums = lax.optimization_barrier((qkv_grad, chip_mixed, got_sums))
    sums = own_sums + got_sums
    got_sums = send_phase(sums, 1)
    chip_halves = call_kernel(
        cut_kernel,
        [((quarter // 2, 4 * channels), low)] * 2,
        [],
        [chip_mixed],
        "v",
        1,
        12,
    )
    both_halves = [send_height(half, 1) for half in chip_halves]
    qkv_grad, proj_grad = call_kernel(
        last_kernel,
        grad_shapes,
        widened(4, quarter // 2),
        [chip_mixed, *both_halves, qkv_grad, proj_grad],
        "vvvhh",
        1,
        12,
        "hh",
        {3: 0, 4: 1},
    )
    qkv_grad, own_total = lax.optimization_barrier((qkv_grad, own_total))
    (input_grad,) = call_kernel(
        own_kernel,
        [((own_pixels, channels), low)],
        [],
        [own_total, partial_sums, all_features, residual_grad, table],
        "vvvvv",
        dot_flops // 4,
        12,
        "o",
    )
    input_grad, got_share, got_sums = lax.optimization_barrier((input_grad, got_share, got_sums))
    vector_shapes = [norm_gains.shape, norm_shifts.shape, conv_biases.shape, qv_bias.shape]
    conv_grad, gains_grad, shifts_grad, biases_grad, qv_grad, proj_bias_grad = call_kernel(
        sums_kernel,
        [((2, 3, 3, out_share, ci_share), wide)]
        + [(shape, wide) for shape in vector_shapes + [(1, channels)]],
        [],
        [sums, got_sums, hold_one, hold_two, got_share],
        "vvvvv",
        1,
        12,
        "o" * 6,
    )
    own_shape = (1, local_rows, cols, channels)
    return (
        output.reshape(own_shape),
        input_grad.reshape(own_shape),
        gains_grad,
        shifts_grad,
        jnp.swapaxes(conv_grad, 3, 4),
        biases_grad,
        qkv_grad,
        qv_grad,
        proj_grad,
        proj_bias_grad.reshape(channels),
    )


def on_device(*arrays):
    features, tile_ids = arrays[0], arrays[1]
    local_rows, cols, channels = features.shape[1:]
    pixels = tile_ids.shape[1] * cols
    height_size, canvas_size = lax.axis_size("height"), lax.axis_size("canvas")
    powers = all(size & (size - 1) == 0 for size in (height_size, canvas_size, cols))
    fits = (
        powers
        and height_size > 2
        and canvas_size == 4
        and channels == LANES * canvas_size
        and pixels <= MOST_PIXELS
        and pixels % FILL_ROWS == 0
        and pixels >= EARLY_ROWS
        and FILL_ROWS % CHUNK == 0
        and pixels % SCORE_ROWS == 0
        and pixels % KEY_ROWS == 0
        and (local_rows * cols) % LANES == 0
        and CHUNK % cols == 0
        and cols % 16 == 0
        and channels % (LANES * canvas_size) == 0
        and 2 * channels == NARROW * height_size
    )
    return whole_canvas(*arrays) if fits else split_canvas(*arrays)


def solution(mesh):
    in_specs = (
        P("canvas", "height", None, None),
        P("canvas", None),
        P(),
        P(),
        P(),
        P(),
        P(),
        P(),
        P(),
        P(),
        P("canvas", "height", None, None),
    )
    out_specs = (
        P("canvas", "height", None, None),
        P("canvas", "height", None, None),
        P(),
        P(),
        P(None, None, None, "canvas", "height"),
        P(),
        P(),
        P(),
        P(),
        P(),
    )
    return jax.shard_map(
        on_device, mesh=mesh, in_specs=in_specs, out_specs=out_specs, check_vma=False
    )
```

```python
import functools

import jax
import jax.numpy as jnp
from jax import lax
from jax.experimental import pallas as pl
from jax.experimental.pallas import tpu as pltpu
from jax.sharding import PartitionSpec as P

GROUPS = 32


epsilon = 1e-06
masked_score = -1e30
MOST_PIXELS = 1024
LANES = 128
NARROW = 128
CHUNK = 128
FILL_ROWS = 256
EARLY_ROWS = 512
SCORE_ROWS = 256
KEY_ROWS = 256


def extended(block, sides, width):
    for axis, dim in sides:
        count = lax.axis_size(axis)
        forward = [(i, i + 1) for i in range(count - 1)]
        backward = [(target, source) for source, target in forward]
        low = lax.ppermute(
            lax.slice_in_dim(block, block.shape[dim] - width, None, axis=dim), axis, forward
        )
        high = lax.ppermute(lax.slice_in_dim(block, 0, width, axis=dim), axis, backward)
        block = jnp.concatenate([low, block, high], axis=dim)
    return block


def group_total(vector):
    return vector.reshape(GROUPS, -1).sum(axis=1)


def spread_groups(vector, channels):
    return jnp.repeat(vector, channels // GROUPS)


def norm_forward(values, gain, shift, members):
    channels = values.shape[1]
    totals = lax.psum(group_total(jnp.sum(values, axis=0)), "height")
    centered = values - spread_groups(totals / members, channels)
    squares = lax.psum(group_total(jnp.sum(centered * centered, axis=0)), "height")
    inverse = spread_groups(lax.rsqrt(squares / members + epsilon), channels)
    normed = centered * inverse
    return (normed, inverse, normed * gain + shift)


def norm_backward(grad_in, normed, inverse, gain, members):
    channels = grad_in.shape[1]
    scaled = grad_in * gain
    both_sums = lax.psum(
        (group_total(jnp.sum(scaled, axis=0)), group_total(jnp.sum(scaled * normed, axis=0))),
        "height",
    )
    mean_grad = spread_groups(both_sums[0] / members, channels)
    mean_cross = spread_groups(both_sums[1] / members, channels)
    result = inverse * (scaled - mean_grad - normed * mean_cross)
    return (result, jnp.sum(grad_in * normed, axis=0), jnp.sum(grad_in, axis=0))


def swish(values):
    return values * jax.nn.sigmoid(values)


def swish_slope(values):
    sigmoid_part = jax.nn.sigmoid(values)
    return sigmoid_part * (1.0 + values * (1.0 - sigmoid_part))


def tap_columns(padded, row_mask, local_rows, canvas_cols):
    pieces = []
    for row_tap in range(3):
        rows_taken = padded[row_tap : row_tap + local_rows] * row_mask[:, row_tap, None, None]
        for col_tap in range(3):
            pieces.append(rows_taken[:, col_tap : col_tap + canvas_cols])
    stacked = jnp.concatenate(pieces, axis=2)
    return stacked.reshape(local_rows * canvas_cols, stacked.shape[2])


def conv_forward(acts, row_mask, weight, bias):
    local_rows, canvas_cols, channels = acts.shape
    rimmed = extended(acts, (("height", 0),), 1)
    padded = jnp.pad(rimmed, ((0, 0), (1, 1), (0, 0)))
    gathered = tap_columns(padded, row_mask, local_rows, canvas_cols)
    result = (
        jnp.dot(
            gathered, weight.reshape(9 * channels, channels), preferred_element_type=jnp.float32
        )
        + bias
    )
    return (result, gathered)


def conv_backward(grad_low, row_mask, weight, gathered):
    local_rows, canvas_cols, channels = grad_low.shape
    flat_grad = grad_low.reshape(local_rows * canvas_cols, channels)
    weight_grad = lax.dot_general(
        gathered, flat_grad, (((0,), (0,)), ((), ())), preferred_element_type=jnp.float32
    )
    rimmed = extended(grad_low, (("height", 0),), 1)
    padded = jnp.pad(rimmed, ((0, 0), (1, 1), (0, 0)))
    grad_taps = tap_columns(padded, row_mask, local_rows, canvas_cols)
    flipped = jnp.transpose(weight[::-1, ::-1], (0, 1, 3, 2)).reshape(9 * channels, channels)
    input_part = jnp.dot(grad_taps, flipped, preferred_element_type=jnp.float32)
    return (
        input_part,
        weight_grad.reshape(3, 3, channels, channels),
        jnp.sum(flat_grad.astype(jnp.float32), axis=0),
    )


def take_rows(array, offset, count):
    return lax.dynamic_slice_in_dim(array, offset, count)


def score_grads(
    queries, out_grad, log_total, row_dots, query_ids, key_rows, value_rows, key_ids, score_scale
):
    scores = (
        lax.dot_general(
            queries, key_rows, (((1,), (1,)), ((), ())), preferred_element_type=jnp.float32
        )
        * score_scale
    )
    same_tile = query_ids[:, None] == key_ids[None, :]
    softmax_block = jnp.exp(jnp.where(same_tile, scores - log_total[:, None], masked_score))
    weight_grad = lax.dot_general(
        out_grad, value_rows, (((1,), (1,)), ((), ())), preferred_element_type=jnp.float32
    )
    score_grad = (softmax_block * (weight_grad - row_dots[:, None])).astype(jnp.bfloat16)
    return (softmax_block.astype(jnp.bfloat16), score_grad)


def split_canvas(
    features,
    tile_ids,
    norm_gains,
    norm_shifts,
    conv_weights,
    conv_biases,
    qkv_weight,
    qv_bias,
    proj_weight,
    proj_bias,
    cotangent,
):
    height_size = lax.axis_size("height")
    local_rows = features.shape[1]
    canvas_cols = features.shape[2]
    channels = features.shape[3]
    pixels = local_rows * canvas_cols
    row_ids = tile_ids[0]
    all_rows = row_ids.shape[0]
    members = float(all_rows * canvas_cols * (channels // GROUPS))
    score_scale = channels ** (-0.5)
    first_row = lax.axis_index("height") * local_rows
    edge_ids = jnp.full((1,), -1, jnp.int32)
    padded_ids = jnp.concatenate([edge_ids, row_ids, edge_ids])
    near_ids = lax.dynamic_slice_in_dim(padded_ids, first_row, local_rows + 2)
    own_rows = near_ids[1 : local_rows + 1]
    row_mask = jnp.stack(
        [near_ids[row_tap : row_tap + local_rows] == own_rows for row_tap in range(3)], axis=1
    ).astype(jnp.bfloat16)
    key_ids = jnp.repeat(row_ids, canvas_cols)
    query_ids = jnp.repeat(own_rows, canvas_cols)
    grid_shape = (local_rows, canvas_cols, channels)
    inputs = features[0].reshape(pixels, channels).astype(jnp.float32)
    normed_one, inverse_one, pre_one = norm_forward(inputs, norm_gains[0], norm_shifts[0], members)
    act_one = swish(pre_one).astype(jnp.bfloat16).reshape(grid_shape)
    middle, taps_one = conv_forward(act_one, row_mask, conv_weights[0], conv_biases[0])
    normed_two, inverse_two, pre_two = norm_forward(middle, norm_gains[1], norm_shifts[1], members)
    act_two = swish(pre_two).astype(jnp.bfloat16).reshape(grid_shape)
    branch, taps_two = conv_forward(act_two, row_mask, conv_weights[1], conv_biases[1])
    residual = inputs + branch
    normed_three, inverse_three, pre_three = norm_forward(
        residual, norm_gains[2], norm_shifts[2], members
    )
    attn_input = pre_three.astype(jnp.bfloat16)
    mixed = jnp.dot(attn_input, qkv_weight, preferred_element_type=jnp.float32)
    queries = (mixed[:, :channels] + qv_bias[0]).astype(jnp.bfloat16)
    key_rows = mixed[:, channels : 2 * channels].astype(jnp.bfloat16)
    value_rows = (mixed[:, 2 * channels :] + qv_bias[1]).astype(jnp.bfloat16)
    running_max = jnp.full((pixels,), masked_score, jnp.float32)
    key_piece = lax.all_gather(key_rows, "height", axis=0, tiled=True)
    value_piece = lax.all_gather(value_rows, "height", axis=0, tiled=True)
    scores = (
        lax.dot_general(
            queries, key_piece, (((1,), (1,)), ((), ())), preferred_element_type=jnp.float32
        )
        * score_scale
    )
    same_tile = query_ids[:, None] == key_ids[None, :]
    scores = jnp.where(same_tile, scores, masked_score)
    new_max = jnp.maximum(running_max, jnp.max(scores, axis=1))
    weights = jnp.where(same_tile, jnp.exp(scores - new_max[:, None]), 0.0)
    summed_out = jnp.dot(
        weights.astype(jnp.bfloat16), value_piece, preferred_element_type=jnp.float32
    )
    total_weight = jnp.sum(weights, axis=1)
    log_total = new_max + jnp.log(total_weight)
    attended = summed_out / total_weight[:, None]
    attended_low = attended.astype(jnp.bfloat16)
    output = (
        residual
        + jnp.dot(attended_low, proj_weight, preferred_element_type=jnp.float32)
        + proj_bias
    )
    out_grad = cotangent[0].reshape(pixels, channels)
    out_grad_full = out_grad.astype(jnp.float32)
    proj_grad = lax.dot_general(
        attended_low, out_grad, (((0,), (0,)), ((), ())), preferred_element_type=jnp.float32
    )
    proj_bias_grad = jnp.sum(out_grad_full, axis=0)
    attended_grad = lax.dot_general(
        out_grad, proj_weight, (((1,), (1,)), ((), ())), preferred_element_type=jnp.float32
    ).astype(jnp.bfloat16)
    row_dots = jnp.sum(attended_grad.astype(jnp.float32) * attended, axis=1)
    block_rows = pixels * min(height_size, 8)
    zero_block = jnp.zeros((pixels, channels), jnp.float32)
    key_all, value_all = (
        lax.all_gather(key_rows, "height", axis=0, tiled=True),
        lax.all_gather(value_rows, "height", axis=0, tiled=True),
    )
    query_all, grad_all = (
        lax.all_gather(queries, "height", axis=0, tiled=True),
        lax.all_gather(attended_grad, "height", axis=0, tiled=True),
    )
    total_all, dots_all = (
        lax.all_gather(log_total, "height", axis=0, tiled=True),
        lax.all_gather(row_dots, "height", axis=0, tiled=True),
    )

    def own_query_step(running, block_index):
        offset = block_index * block_rows
        key_part = take_rows(key_all, offset, block_rows)
        rounded, score_grad = score_grads(
            queries,
            attended_grad,
            log_total,
            row_dots,
            query_ids,
            key_part,
            take_rows(value_all, offset, block_rows),
            take_rows(key_ids, offset, block_rows),
            score_scale,
        )
        return (
            running
            + jnp.dot(score_grad, key_part, preferred_element_type=jnp.float32) * score_scale,
            None,
        )

    def own_key_step(running, block_index):
        offset = block_index * block_rows
        query_part = take_rows(query_all, offset, block_rows)
        grad_part = take_rows(grad_all, offset, block_rows)
        rounded, score_grad = score_grads(
            query_part,
            grad_part,
            take_rows(total_all, offset, block_rows),
            take_rows(dots_all, offset, block_rows),
            take_rows(key_ids, offset, block_rows),
            key_rows,
            value_rows,
            query_ids,
            score_scale,
        )
        key_part = (
            lax.dot_general(
                score_grad, query_part, (((0,), (0,)), ((), ())), preferred_element_type=jnp.float32
            )
            * score_scale
        )
        value_part = lax.dot_general(
            rounded, grad_part, (((0,), (0,)), ((), ())), preferred_element_type=jnp.float32
        )
        return ((running[0] + key_part, running[1] + value_part), None)

    block_count = key_all.shape[0] // block_rows
    query_grad, unused_one = lax.scan(own_query_step, zero_block, jnp.arange(block_count))
    (key_grad, value_grad), unused_two = lax.scan(
        own_key_step, (zero_block, zero_block), jnp.arange(block_count)
    )
    query_low = query_grad.astype(jnp.bfloat16)
    key_low = key_grad.astype(jnp.bfloat16)
    value_low = value_grad.astype(jnp.bfloat16)
    stacked_grad = jnp.concatenate([query_low, key_low, value_low], axis=1)
    qkv_grad = lax.dot_general(
        attn_input, stacked_grad, (((0,), (0,)), ((), ())), preferred_element_type=jnp.float32
    )
    qv_grad = jnp.stack(
        [
            jnp.sum(query_low.astype(jnp.float32), axis=0),
            jnp.sum(value_low.astype(jnp.float32), axis=0),
        ]
    )
    normed_grad = lax.dot_general(
        stacked_grad, qkv_weight, (((1,), (1,)), ((), ())), preferred_element_type=jnp.float32
    )
    back_three, gain_three, shift_three = norm_backward(
        normed_grad, normed_three, inverse_three, norm_gains[2], members
    )
    residual_grad = out_grad_full + back_three
    grad_two = residual_grad.astype(jnp.bfloat16).reshape(grid_shape)
    act_two_grad, weight_two_grad, bias_two_grad = conv_backward(
        grad_two, row_mask, conv_weights[1], taps_two
    )
    middle_grad, gain_two, shift_two = norm_backward(
        act_two_grad * swish_slope(pre_two), normed_two, inverse_two, norm_gains[1], members
    )
    grad_one = middle_grad.astype(jnp.bfloat16).reshape(grid_shape)
    act_one_grad, weight_one_grad, bias_one_grad = conv_backward(
        grad_one, row_mask, conv_weights[0], taps_one
    )
    input_back, gain_one, shift_one = norm_backward(
        act_one_grad * swish_slope(pre_one), normed_one, inverse_one, norm_gains[0], members
    )
    input_grad = residual_grad + input_back
    conv_grad = jnp.stack([weight_one_grad, weight_two_grad])
    conv_part = lax.psum_scatter(conv_grad, "height", scatter_dimension=4, tiled=True)
    conv_part = lax.psum_scatter(
        conv_part.astype(jnp.bfloat16), "canvas", scatter_dimension=3, tiled=True
    ).astype(jnp.float32)
    summed = lax.psum(
        (
            jnp.stack([gain_one, gain_two, gain_three]),
            jnp.stack([shift_one, shift_two, shift_three]),
            jnp.stack([bias_one_grad, bias_two_grad]),
            qkv_grad,
            qv_grad,
            proj_grad,
            proj_bias_grad,
        ),
        ("canvas", "height"),
    )
    return (
        output.astype(jnp.bfloat16).reshape((1,) + grid_shape),
        input_grad.astype(jnp.bfloat16).reshape((1,) + grid_shape),
        summed[0],
        summed[1],
        conv_part,
        summed[2],
        summed[3],
        summed[4],
        summed[5],
        summed[6],
    )


def fold(block):
    rows, width = block.shape
    return jnp.sum(block.reshape(rows // 8, 8, width), axis=0)


def group_lanes(block, group):
    lane = lax.broadcasted_iota(jnp.int32, block.shape, 1)
    width = block.shape[1]
    step = 1
    while step < group:
        above = pltpu.roll(block, step, 1)
        below = pltpu.roll(block, width - step, 1)
        block = block + jnp.where((lane & step) != 0, above, below)
        step *= 2
    return block


def group_mean(partial, members):
    spread = group_lanes(partial, partial.shape[1] // GROUPS)
    return jnp.sum(spread, axis=0, keepdims=True) * (1.0 / members)


def widen(block, width):
    return jnp.concatenate([block] * (width // block.shape[1]), axis=1)


def each_block(pixels, block, body, carry=0):
    def step(index, carry):
        return body(pl.ds(pl.multiple_of(index * block, block), block), carry)

    return lax.fori_loop(0, pixels // block, step, carry)


def each_chunk(pixels, body, carry):
    return each_block(pixels, CHUNK, body, carry)


def aligned(start, step):
    return start if isinstance(start, int) else pl.multiple_of(start, step)


class RunningStats:
    def __init__(self, channels):
        self.width = channels // GROUPS
        self.reference = None
        self.sums = self.squares = jnp.zeros((8, channels), jnp.float32)

    def add(self, block):
        if self.reference is None:
            self.reference = group_mean(block[0:8], 8.0 * self.width)
        offset = block - self.reference
        self.sums = self.sums + fold(offset)
        self.squares = self.squares + fold(offset * offset)

    def finish(self, pixels):
        both = group_lanes(jnp.concatenate([self.sums, self.squares], axis=0), self.width)
        share = 1.0 / (pixels * self.width)
        offset = column_total(both[0:8]) * share
        variance = column_total(both[8:16]) * share - offset * offset
        return self.reference + offset, lax.rsqrt(jnp.maximum(variance, 0.0) + epsilon)


def put_taps(taps_ref, block, rows, cols):
    count, channels = block.shape
    place = lax.broadcasted_iota(jnp.int32, block.shape, 0) & (cols - 1)
    left = jnp.where(place == 0, 0.0, pltpu.roll(block, 1, 0))
    right = jnp.where(place == cols - 1, 0.0, pltpu.roll(block, count - 1, 0))
    inner = pl.ds(aligned(rows.start + cols, cols), count)
    taps_ref[inner, 0:channels] = left.astype(jnp.bfloat16)
    taps_ref[inner, channels : 2 * channels] = block.astype(jnp.bfloat16)
    taps_ref[inner, 2 * channels :] = right.astype(jnp.bfloat16)


def clear_edges(taps_ref, cols):
    edge = jnp.zeros((cols, taps_ref.shape[1]), taps_ref.dtype)
    taps_ref[0:cols, :] = edge
    taps_ref[taps_ref.shape[0] - cols :, :] = edge


def begin_conv(taps_ref, product, total_ref, fill, first, cols):
    for start in range(0, total_ref.shape[0], FILL_ROWS):
        for inner in range(start, start + FILL_ROWS, CHUNK):
            fill(pl.ds(inner, CHUNK))
        rows = pl.ds(start, FILL_ROWS)
        total_ref[rows, :] = first(rows, product(taps_ref, pl.ds(start + cols, FILL_ROWS), 1))


def add_rows(taps_ref, product, mask_ref, total_ref, stop, cols):
    rows = pl.ds(0, stop)
    part = product(taps_ref, rows, 0)
    total_ref[rows, :] += widen(mask_ref[0, rows, :], total_ref.shape[1]) * part


def end_conv(taps_ref, product, mask_ref, total_ref, last, cols, old_ref=None, pending=None):
    pixels, channels = total_ref.shape
    old_ref = total_ref if old_ref is None else old_ref
    pending = pixels if pending is None else pending
    for start in range(0, pixels, FILL_ROWS):
        rows = pl.ds(start, FILL_ROWS)
        value = old_ref[rows, :]
        for row_tap in (0, 2) if start >= pending else (2,):
            part = product(taps_ref, pl.ds(start + row_tap * cols, FILL_ROWS), row_tap)
            value = value + widen(mask_ref[row_tap // 2, rows, :], channels) * part
        total_ref[rows, :] = last(rows, value)


def run_conv(taps_ref, product, mask_ref, total_ref, fill, first, last, cols):
    begin_conv(taps_ref, product, total_ref, fill, first, cols)
    add_rows(taps_ref, product, mask_ref, total_ref, total_ref.shape[0], cols)
    end_conv(taps_ref, product, mask_ref, total_ref, last, cols)


def product_forward(weight_ref):
    channels = weight_ref.shape[-1]

    def product(taps_ref, shifted, row_tap):
        return jnp.dot(
            taps_ref[shifted, :],
            weight_ref[row_tap].reshape(3 * channels, channels),
            preferred_element_type=jnp.float32,
        )

    return product


def product_backward(weight_ref):
    def product(taps_ref, shifted, row_tap):
        return lax.dot_general(
            taps_ref[shifted, :],
            weight_ref[row_tap],
            (((1,), (1,)), ((), ())),
            preferred_element_type=jnp.float32,
        )

    return product


def activation(read, mean, inverse, gain, shift, act_ref, taps_ref, cols):
    scale, offset = 0.5 * inverse * gain, 0.5 * shift

    def fill(rows):
        half = (read(rows) - mean) * scale + offset
        act = half * (1.0 + jnp.tanh(half))
        act_ref[rows, :] = act.astype(jnp.bfloat16)
        put_taps(taps_ref, act, rows, cols)

    return fill


def back_means(sums, gain, pixels):
    channels = gain.shape[1]
    members = float(pixels * (channels // GROUPS))
    return group_mean(sums[0] * gain, members), group_mean(sums[1] * gain, members)


def column_total(partial):
    return jnp.sum(partial, axis=0, keepdims=True)


def weight_part(act_ref, narrow, lanes_ref, flip_ref, columns_ref, part_ref, cols):
    pixels, channels = act_ref.shape
    height = lax.axis_index("height")
    share = NARROW // 2
    flip_ref[...] = narrow.T
    own = pl.ds(pl.multiple_of((height % 2) * share, share), share)
    grad = flip_ref[own, :].astype(jnp.float32)
    column = lax.broadcasted_iota(jnp.int32, grad.shape, 1) & (cols - 1)
    for col_tap in range(3):
        shifted = grad
        if col_tap == 0:
            shifted = jnp.where(column == cols - 1, 0.0, pltpu.roll(grad, pixels - 1, 1))
        elif col_tap == 2:
            shifted = jnp.where(column == 0, 0.0, pltpu.roll(grad, 1, 1))
        for row_tap in range(3):
            tap = 3 * row_tap + col_tap
            place = slice(tap * share, (tap + 1) * share)
            if row_tap == 1:
                columns_ref[place, :] = shifted.astype(jnp.bfloat16)
                continue
            side, turn = (0, pixels - cols) if row_tap == 0 else (1, cols)
            masked = (shifted * lanes_ref[side : side + 1, :]).astype(jnp.bfloat16)
            columns_ref[place, :] = pltpu.roll(masked, turn, 1)
    part_ref[...] = jnp.dot(
        columns_ref[...], act_ref[...], preferred_element_type=jnp.float32
    ).astype(jnp.bfloat16)


def begin_back(read, weights_ref, mask_ref, taps_ref, total_ref, stop, cols):
    clear_edges(taps_ref, cols)

    def fill(rows):
        put_taps(taps_ref, read(rows), rows, cols)

    product = product_backward(weights_ref)
    begin_conv(taps_ref, product, total_ref, fill, lambda rows, part: part, cols)
    if stop:
        add_rows(taps_ref, product, mask_ref, total_ref, stop, cols)


def finish_back(
    weights_ref,
    mask_ref,
    taps_ref,
    total_ref,
    read,
    table_ref,
    which,
    cols,
    old_ref=None,
    pending=None,
):
    mean, inverse, gain, shift = norm_rows(table_ref, which)
    scale, offset = 0.5 * inverse * gain, 0.5 * shift
    sums = []

    def slope(rows, value):
        centered = read(rows) - mean
        half = centered * scale + offset
        turn = jnp.tanh(half)
        double = value * ((1.0 + turn) * (1.0 + half * (1.0 - turn)))
        sums.append((fold(double), fold(double * centered)))
        return double

    product = product_backward(weights_ref)
    end_conv(taps_ref, product, mask_ref, total_ref, slope, cols, old_ref, pending)
    plain, cross = sum(pair[0] for pair in sums), sum(pair[1] for pair in sums)
    return 0.5 * plain, 0.5 * inverse * cross


def norm_back(total_ref, double, sums, read, table_ref, which, pixels, scales_ref=None):
    mean, inverse, gain, shift = norm_rows(table_ref, which)
    mean_grad, mean_cross = back_means(sums, gain, pixels)
    slope = inverse * gain * (0.5 if double else 1.0)
    level, tilt = inverse * mean_grad, inverse * inverse * mean_cross
    if scales_ref is not None:
        for row, scales in enumerate((mean, slope, level, tilt)):
            scales_ref[row : row + 1, :] = scales

    def back(rows, inner):
        return total_ref[inner, :] * slope - level - (read(rows) - mean) * tilt

    return back


def own_lanes():
    block = lax.axis_index("height") // 2
    return pl.ds(pl.multiple_of(block * NARROW, NARROW), NARROW)


def narrow_back(total_ref, value_ref, scales_ref):
    lanes = own_lanes()
    mean, slope, level, tilt = (scales_ref[row : row + 1, lanes] for row in range(4))
    return total_ref[:, lanes] * slope - level - (value_ref[:, lanes] - mean) * tilt


def scaled_back(total_ref, value_ref, scales_ref, rows, inner):
    mean, slope, level, tilt = (scales_ref[row : row + 1, :] for row in range(4))
    return total_ref[inner, :] * slope - level - (value_ref[rows, :].astype(jnp.float32) - mean) * tilt


def turn_kernel(
    grad_ref,
    total_three_ref,
    scales_ref,
    residual_ref,
    mask_ref,
    weights_ref,
    old_sums_ref,
    total_ref,
    taps_ref,
    sums_ref,
    *,
    cols,
):
    grad_sums = []

    def read(rows):
        grad = scaled_back(total_three_ref, residual_ref, scales_ref, rows, rows)
        grad = grad_ref[rows, :].astype(jnp.float32) + grad
        grad = grad.astype(jnp.bfloat16).astype(jnp.float32)
        grad_sums.append(fold(grad))
        return grad

    begin_back(read, weights_ref.at[1], mask_ref, taps_ref, total_ref, EARLY_ROWS, cols)
    sums_ref[...] = old_sums_ref[...]
    sums_ref[7:8, :] = column_total(sum(grad_sums))


def norm_rows(table_ref, which):
    picks = (2 * which, 2 * which + 1, 6 + which, 9 + which)
    return tuple(table_ref[pick : pick + 1, :] for pick in picks)


def build_masks(ids_ref, mask_ref, lanes_ref, id_rows_ref, id_cols_ref, cols):
    rows = ids_ref.shape[1]

    def one_row(row, carry):
        here = ids_ref[0, row]
        place = pl.ds(pl.multiple_of(row * cols, cols), cols)
        id_rows_ref[place, :] = jnp.full((cols, LANES), here, jnp.int32)
        for side, other in ((0, row - 1), (1, row + 1)):
            inside = jnp.logical_and(other >= 0, other < rows)
            other_id = ids_ref[0, jnp.clip(other, 0, rows - 1)]
            same = jnp.where(jnp.logical_and(inside, other_id == here), 1.0, 0.0)
            mask_ref[side, place, :] = jnp.full((cols, LANES), same, jnp.float32)
        return carry

    lax.fori_loop(0, rows, one_row, 0)
    lane = lax.broadcasted_iota(jnp.int32, (8, LANES), 1)
    each = LANES // cols
    for block in range(rows // each):
        ids = jnp.full((8, LANES), ids_ref[0, block * each], jnp.int32)
        for step in range(1, each):
            ids = jnp.where(lane >= step * cols, ids_ref[0, block * each + step], ids)
        id_cols_ref[:, block * LANES : (block + 1) * LANES] = ids
    ids = id_cols_ref[...].astype(jnp.float32)
    pixels = ids.shape[1]
    pixel = lax.broadcasted_iota(jnp.int32, ids.shape, 1)
    above = jnp.where(pixel < cols, -1.0, pltpu.roll(ids, cols, 1))
    below = jnp.where(pixel >= pixels - cols, -1.0, pltpu.roll(ids, pixels - cols, 1))
    lanes_ref[0:1, :] = jnp.where(above == ids, 1.0, 0.0)[0:1]
    lanes_ref[1:2, :] = jnp.where(below == ids, 1.0, 0.0)[0:1]


def place_pieces(pieces, whole_ref, sems):
    own_pixels = whole_ref.shape[0] // len(pieces)
    height = lax.axis_index("height")
    copies = []
    for place, piece in enumerate(pieces):
        piece = piece.at[piece.shape[0] - own_pixels : piece.shape[0], :]
        start = pl.multiple_of((height ^ place) * own_pixels, own_pixels)
        rows = pl.ds(start, own_pixels)
        copies.append(pltpu.make_async_copy(piece, whole_ref.at[rows, :], sems.at[place]))
    return copies


def hold_kernel(
    ids_hbm,
    gains_hbm,
    shifts_hbm,
    biases_hbm,
    weights_hbm,
    qkv_hbm,
    proj_hbm,
    qv_bias_hbm,
    proj_bias_hbm,
    weights_ref,
    turned_ref,
    qkv_ref,
    proj_ref,
    table_ref,
    mask_ref,
    lanes_ref,
    id_rows_ref,
    id_cols_ref,
    ids_ref,
    gains_ref,
    shifts_ref,
    biases_ref,
    qv_bias_ref,
    proj_bias_ref,
    sems,
    *,
    cols,
):
    channels = weights_ref.shape[-1]
    small = [
        (ids_hbm, ids_ref),
        (gains_hbm, gains_ref),
        (shifts_hbm, shifts_ref),
        (biases_hbm, biases_ref),
        (qv_bias_hbm, qv_bias_ref),
        (proj_bias_hbm, proj_bias_ref),
    ]
    large = [(weights_hbm, weights_ref), (qkv_hbm, qkv_ref), (proj_hbm, proj_ref)]
    for which in range(2):
        for row_tap in range(3):
            for col_tap in range(3):
                place = slice(col_tap * channels, (col_tap + 1) * channels)
                large.append(
                    (
                        weights_hbm.at[which, 2 - row_tap, 2 - col_tap],
                        turned_ref.at[which, row_tap, :, place],
                    )
                )
    copies = [
        pltpu.make_async_copy(source, target, sems.at[index])
        for index, (source, target) in enumerate(small + large)
    ]
    for copy in copies:
        copy.start()
    for copy in copies[: len(small)]:
        copy.wait()
    build_masks(ids_ref, mask_ref, lanes_ref, id_rows_ref, id_cols_ref, cols)
    table_ref[6:9, :] = gains_ref[...]
    table_ref[9:12, :] = shifts_ref[...]
    table_ref[12:14, :] = biases_ref[...]
    table_ref[14:16, :] = qv_bias_ref[...]
    table_ref[16:17, :] = proj_bias_ref[...]
    for copy in copies[len(small) :]:
        copy.wait()


def conv_kernel(*refs, cols, count):
    pieces, refs = refs[:count], refs[count:]
    (
        weights_ref,
        params_ref,
        mask_ref,
        features_ref,
        act_one_ref,
        middle_ref,
        act_two_ref,
        residual_ref,
        table_ref,
        own_ref,
        taps_ref,
        sem,
    ) = refs
    pixels, channels = features_ref.shape
    wide = jnp.float32
    own_copy = pltpu.make_async_copy(pieces[0], own_ref, sem)
    own_copy.start()
    table_ref[...] = params_ref[...]
    clear_edges(taps_ref, cols)

    def read_input(rows):
        return features_ref[rows, :].astype(wide)

    def read_middle(rows):
        return middle_ref[rows, :]

    height = lax.axis_index("height")
    own_pixels = pixels // count
    seen = RunningStats(channels)
    for place in list(range(1, count)) + [0]:
        if place == 0:
            own_copy.wait()
        piece = (pieces[place] if place else own_ref)[0:own_pixels, :]
        start = pl.multiple_of((height ^ place) * own_pixels, own_pixels)
        features_ref[pl.ds(start, own_pixels), :] = piece
        seen.add(piece.astype(wide))
    table_ref[0:1, :], table_ref[1:2, :] = seen.finish(pixels)
    seen = RunningStats(channels)

    def keep(rows, value):
        seen.add(value)
        return value

    run_conv(
        taps_ref,
        product_forward(weights_ref.at[0]),
        mask_ref,
        middle_ref,
        activation(read_input, *norm_rows(table_ref, 0), act_one_ref, taps_ref, cols),
        lambda rows, part: part + table_ref[12:13, :],
        keep,
        cols,
    )
    table_ref[2:3, :], table_ref[3:4, :] = seen.finish(pixels)
    seen = RunningStats(channels)
    run_conv(
        taps_ref,
        product_forward(weights_ref.at[1]),
        mask_ref,
        residual_ref,
        activation(read_middle, *norm_rows(table_ref, 1), act_two_ref, taps_ref, cols),
        lambda rows, part: part + (read_input(rows) + table_ref[13:14, :]),
        keep,
        cols,
    )
    table_ref[4:5, :], table_ref[5:6, :] = seen.finish(pixels)


def score_kernel(
    qkv_ref,
    proj_ref,
    residual_ref,
    table_ref,
    id_rows_ref,
    id_cols_ref,
    normed_ref,
    query_ref,
    key_ref,
    value_ref,
    soft_ref,
    out_flip_ref,
    output_ref,
    value_flip_ref,
    *scores_refs,
    score_scale,
):
    pixels, channels = residual_ref.shape
    own_pixels = output_ref.shape[0]
    wide = jnp.float32
    exponent = score_scale * 1.4426950408889634
    mean, inverse, gain, shift = norm_rows(table_ref, 2)
    scale = inverse * gain

    def normalise(start):
        rows = slice(start, start + KEY_ROWS)
        normed = (residual_ref[rows, :] - mean) * scale + shift
        normed_ref[rows, :] = normed.astype(jnp.bfloat16)

    def project(start):
        rows = slice(start, start + KEY_ROWS)
        normed = normed_ref[rows, :]
        query_ref[rows, :] = (
            jnp.dot(normed, qkv_ref[:, 0:channels], preferred_element_type=wide)
            + table_ref[14:15, :]
        ).astype(jnp.bfloat16)
        key_ref[rows, :] = jnp.dot(
            normed, qkv_ref[:, channels : 2 * channels], preferred_element_type=wide
        ).astype(jnp.bfloat16)
        values = (
            jnp.dot(normed, qkv_ref[:, 2 * channels :], preferred_element_type=wide)
            + table_ref[15:16, :]
        ).astype(jnp.bfloat16)
        value_ref[rows, :] = values
        value_flip_ref[:, rows] = values.T

    normalise(0)
    for start in range(0, pixels, KEY_ROWS):
        if start + KEY_ROWS < pixels:
            normalise(start + KEY_ROWS)
        project(start)
    block = scores_refs[0].shape[1]
    steps = range(0, pixels, KEY_ROWS)

    def score(index):
        rows = slice(index * block, (index + 1) * block)
        for start in steps:
            keys = slice(start, start + KEY_ROWS)
            scores = lax.dot_general(
                key_ref[keys, :],
                query_ref[rows, :],
                (((1,), (1,)), ((), ())),
                preferred_element_type=wide,
            )
            same = widen(id_rows_ref[keys, :], block) == id_cols_ref[0:1, rows]
            scores_refs[index][keys, :] = jnp.where(same, scores, masked_score)

    def soften(index):
        rows = slice(index * block, (index + 1) * block)
        scores_ref = scores_refs[index]
        peak = jnp.full((8, block), masked_score, wide)
        for start in steps:
            scores = scores_ref[start : start + KEY_ROWS, :]
            peak = jnp.maximum(peak, jnp.max(scores.reshape(-1, 8, block), axis=0))
        peak = jnp.max(peak, axis=0, keepdims=True)
        total = jnp.zeros((8, block), wide)
        for start in steps:
            keys = slice(start, start + KEY_ROWS)
            powers = jnp.exp2((scores_ref[keys, :] - peak) * exponent)
            scores_ref[keys, :] = powers
            total = total + fold(powers)
        share = 1.0 / column_total(total)
        for start in steps:
            keys = slice(start, start + KEY_ROWS)
            soft_ref[keys, rows] = (scores_ref[keys, :] * share).astype(jnp.bfloat16)

    score(0)
    for index in range(len(scores_refs)):
        if index + 1 < len(scores_refs):
            score(index + 1)
        soften(index)
        rows = slice(index * block, (index + 1) * block)
        out_flip_ref[:, rows] = jnp.dot(
            value_flip_ref[...], soft_ref[:, rows], preferred_element_type=wide
        ).astype(jnp.bfloat16)
    height = lax.axis_index("height")
    own = pl.ds(pl.multiple_of(height * own_pixels, own_pixels), own_pixels)
    output_ref[...] = (
        residual_ref[own, :]
        + lax.dot_general(
            out_flip_ref[:, own],
            proj_ref[...],
            (((0,), (0,)), ((), ())),
            preferred_element_type=wide,
        )
        + table_ref[16:17, :]
    ).astype(jnp.bfloat16)


def own_quarter():
    height = lax.axis_index("height")
    return (height & 1) * 2 + ((height >> 1) & 1)


def attention_kernel(
    proj_ref,
    normed_ref,
    query_ref,
    key_ref,
    value_ref,
    soft_ref,
    out_flip_ref,
    *refs,
    score_scale,
    count,
):
    pieces, (grad_ref, packed_ref, sums_ref), refs = (
        refs[:count],
        refs[count : count + 3],
        refs[count + 3 :],
    )
    pixels, channels = normed_ref.shape
    blocks = pixels // SCORE_ROWS
    grads_refs, refs = refs[-blocks:], refs[:-blocks]
    *mixed_refs, mixed_ref, key_flip_ref, back_ref, score_grad_ref, flip_ref, sems = refs
    wide = jnp.float32
    copies = place_pieces(pieces, grad_ref, sems)
    for copy in copies:
        copy.start()
    quarter = channels // 4
    own = pl.ds(pl.multiple_of(own_quarter() * quarter, quarter), quarter)
    flip_ref[...] = normed_ref[:, own].T
    key_flip_ref[...] = key_ref[...].T
    for copy in copies:
        copy.wait()
    block, count = SCORE_ROWS, blocks
    steps = range(0, pixels, KEY_ROWS)

    def block_rows(index):
        return slice(index * block, (index + 1) * block)

    for start in range(0, pixels, 2 * block):
        rows = slice(start, start + 2 * block)
        back_ref[rows, :] = lax.dot_general(
            grad_ref[rows, :],
            proj_ref[...],
            (((1,), (1,)), ((), ())),
            preferred_element_type=wide,
        ).astype(jnp.bfloat16)

    def weigh(index):
        total = jnp.zeros((8, block), wide)
        for start in steps:
            keys = slice(start, start + KEY_ROWS)
            weight_grad = lax.dot_general(
                value_ref[keys, :],
                back_ref[block_rows(index), :],
                (((1,), (1,)), ((), ())),
                preferred_element_type=wide,
            )
            grads_refs[index][keys, :] = weight_grad
            total = total + fold(soft_ref[keys, block_rows(index)].astype(wide) * weight_grad)
        return column_total(total)

    def slope(index, dots):
        for start in steps:
            keys = slice(start, start + KEY_ROWS)
            weights = soft_ref[keys, block_rows(index)].astype(wide)
            score_grad_ref[keys, block_rows(index)] = (
                weights * (grads_refs[index][keys, :] - dots)
            ).astype(jnp.bfloat16)

    dots = weigh(0)
    for index in range(count):
        now, rows = dots, block_rows(index)
        if index + 1 < count:
            dots = weigh(index + 1)
        slope(index, now)
        packed_ref[rows, 2 * channels :] = jnp.dot(
            soft_ref[rows, :], back_ref[...], preferred_element_type=wide
        ).astype(jnp.bfloat16)
        query_grad = jnp.dot(
            key_flip_ref[...], score_grad_ref[:, rows], preferred_element_type=wide
        )
        packed_ref[rows, 0:channels] = (query_grad * score_scale).astype(jnp.bfloat16).T
    for start in range(0, pixels, 2 * block):
        rows = slice(start, start + 2 * block)
        packed_ref[rows, channels : 2 * channels] = (
            jnp.dot(score_grad_ref[rows, :], query_ref[...], preferred_element_type=wide)
            * score_scale
        ).astype(jnp.bfloat16)

    def pack(rows, carry):
        return (
            carry[0] + fold(packed_ref[rows, 0:channels].astype(wide)),
            carry[1] + fold(packed_ref[rows, 2 * channels :].astype(wide)),
            carry[2] + fold(grad_ref[rows, :].astype(wide)),
        )

    zeros = jnp.zeros((8, channels), wide)
    totals = zeros, zeros, zeros
    for start in range(0, pixels, CHUNK):
        totals = pack(pl.ds(start, CHUNK), totals)
    sums_ref[...] = jnp.zeros(sums_ref.shape, wide)
    for row, total in enumerate(totals):
        sums_ref[8 + row : 9 + row, :] = column_total(total)
    mixed_ref[:, 0 : 3 * channels] = jnp.dot(
        flip_ref[...], packed_ref[...], preferred_element_type=wide
    ).astype(jnp.bfloat16)
    mixed_ref[:, 3 * channels :] = jnp.dot(
        out_flip_ref[own, :], grad_ref[...], preferred_element_type=wide
    ).astype(jnp.bfloat16)
    share = quarter // len(mixed_refs)
    me = lax.axis_index("canvas")
    for step, target in enumerate(mixed_refs):
        target[...] = mixed_ref[pl.ds(pl.multiple_of((me ^ step) * share, share), share), :]


def third_kernel(
    qkv_ref,
    grad_ref,
    packed_ref,
    residual_ref,
    table_ref,
    act_two_ref,
    lanes_ref,
    old_sums_ref,
    total_ref,
    scales_ref,
    sums_ref,
    part_ref,
    flip_ref,
    columns_ref,
    *,
    cols,
):
    pixels, channels = residual_ref.shape
    block = 2 * FILL_ROWS
    wide = jnp.float32
    mean, inverse, gain, shift = norm_rows(table_ref, 2)
    zeros = jnp.zeros((8, channels), wide)

    sums = (zeros, zeros)
    for start in range(0, pixels, block):
        rows = pl.ds(start, block)
        normed_grad = lax.dot_general(
            packed_ref[rows, :], qkv_ref[...], (((1,), (1,)), ((), ())), preferred_element_type=wide
        )
        total_ref[rows, :] = normed_grad
        centered = residual_ref[rows, :] - mean
        sums = sums[0] + fold(normed_grad), sums[1] + fold(normed_grad * centered)
    sums = sums[0], sums[1] * inverse
    sums_ref[...] = old_sums_ref[...]
    sums_ref[5:6, :] = column_total(sums[1])
    sums_ref[6:7, :] = column_total(sums[0])
    norm_back(
        total_ref, False, sums, lambda rows: residual_ref[rows, :], table_ref, 2, pixels, scales_ref
    )
    narrow = narrow_back(total_ref, residual_ref, scales_ref)
    narrow = (grad_ref[:, own_lanes()].astype(wide) + narrow).astype(jnp.bfloat16)
    weight_part(act_two_ref, narrow, lanes_ref, flip_ref, columns_ref, part_ref, cols)


def second_kernel(
    old_total_ref,
    taps_ref,
    middle_ref,
    table_ref,
    act_one_ref,
    mask_ref,
    lanes_ref,
    weights_ref,
    old_sums_ref,
    part_two_ref,
    total_ref,
    scales_ref,
    sums_ref,
    keep_one_ref,
    send_one_ref,
    keep_two_ref,
    send_two_ref,
    flip_ref,
    columns_ref,
    part_ref,
    *,
    cols,
):
    pixels, channels = middle_ref.shape

    def read(rows):
        return middle_ref[rows, :]

    sums = finish_back(
        weights_ref.at[1],
        mask_ref,
        taps_ref,
        total_ref,
        read,
        table_ref,
        1,
        cols,
        old_total_ref,
        EARLY_ROWS,
    )
    norm_back(total_ref, True, sums, read, table_ref, 1, pixels, scales_ref)
    narrow = narrow_back(total_ref, middle_ref, scales_ref).astype(jnp.bfloat16)
    weight_part(act_one_ref, narrow, lanes_ref, flip_ref, columns_ref, part_ref, cols)
    sums_ref[...] = old_sums_ref[...]
    sums_ref[2:3, :] = column_total(sums[1])
    sums_ref[3:4, :] = column_total(sums[0])
    keep_half(part_ref, keep_one_ref, send_one_ref)
    keep_half(part_two_ref, keep_two_ref, send_two_ref)


def near_far():
    core = lax.axis_index("height") & 1
    return 1 + core, 2 - core


def keep_half(source_ref, keep_ref, send_ref):
    me = lax.axis_index("canvas")
    near, far = near_far()
    rows, width = keep_ref.shape[0] // 2, keep_ref.shape[1]
    for target_ref, flip in ((keep_ref, 0), (send_ref, near)):
        for slot, other in enumerate((0, far)):
            place = pl.ds(pl.multiple_of((me ^ flip ^ other) * width, width), width)
            target_ref[slot * rows : (slot + 1) * rows, :] = source_ref[:, place]


def first_kernel(
    total_two_ref,
    scales_ref,
    middle_ref,
    features_ref,
    table_ref,
    mask_ref,
    old_sums_ref,
    weights_ref,
    own_ref,
    sums_ref,
    partial_ref,
    total_ref,
    taps_ref,
    *,
    cols,
):
    def read(rows):
        return features_ref[rows, :].astype(jnp.float32)

    grad_sums = []

    def read_grad(rows):
        grad = scaled_back(total_two_ref, middle_ref, scales_ref, rows, rows)
        grad = grad.astype(jnp.bfloat16).astype(jnp.float32)
        grad_sums.append(fold(grad))
        return grad

    weights = weights_ref.at[0]
    begin_back(read_grad, weights, mask_ref, taps_ref, total_ref, total_ref.shape[0], cols)
    sums = finish_back(weights, mask_ref, taps_ref, total_ref, read, table_ref, 0, cols)
    partial_ref[0:8, :], partial_ref[8:16, :] = sums
    sums_ref[...] = old_sums_ref[...]
    sums_ref[0:1, :] = column_total(sums[1])
    sums_ref[1:2, :] = column_total(sums[0])
    sums_ref[4:5, :] = column_total(sum(grad_sums))
    count = own_ref.shape[0]
    own = pl.ds(pl.multiple_of(lax.axis_index("height") * count, count), count)
    own_ref[...] = total_ref[own, :]


def own_kernel(
    own_ref,
    partial_ref,
    features_ref,
    grad_ref,
    total_three_ref,
    residual_ref,
    scales_ref,
    table_ref,
    input_grad_ref,
):
    def read(rows):
        return features_ref[rows, :].astype(jnp.float32)

    sums = partial_ref[0:8, :], partial_ref[8:16, :]
    pixels = features_ref.shape[0]
    back = norm_back(own_ref, True, sums, read, table_ref, 0, pixels)
    count = own_ref.shape[0]
    own = pl.ds(pl.multiple_of(lax.axis_index("height") * count, count), count)
    total = scaled_back(total_three_ref, residual_ref, scales_ref, own, own)
    total = grad_ref[own, :].astype(jnp.float32) + total
    input_grad_ref[...] = (total + back(own, slice(0, count))).astype(jnp.bfloat16)


def place_kernel(*refs):
    joints, packed_ref = refs[:-1], refs[-1]
    share = packed_ref.shape[0] // len(joints)
    me = lax.axis_index("canvas")
    for step, joint in enumerate(joints):
        place = pl.ds(pl.multiple_of((me ^ step) * share, share), share)
        packed_ref[place, :] = joint[...]


def cut_kernel(packed_ref, *half_refs):
    rows = half_refs[0].shape[0]
    for index, half_ref in enumerate(half_refs):
        half_ref[...] = packed_ref[index * rows : (index + 1) * rows, :]


def spread_quarters(packed, flips, qkv_ref, proj_ref, qkv_hbm, proj_hbm, sems):
    quarter = packed[0].shape[0]
    inner = qkv_ref.shape[2]
    copies = []
    for index, packed_ref in enumerate(packed):
        owner = own_quarter() ^ flips[index]
        rows = pl.ds(pl.multiple_of(owner * quarter, quarter), quarter)
        qkv_ref[index] = packed_ref[:, 0:inner].astype(jnp.float32)
        proj_ref[index] = packed_ref[:, inner:].astype(jnp.float32)
        for which, (held, target) in enumerate(((qkv_ref, qkv_hbm), (proj_ref, proj_hbm))):
            copy = pltpu.make_async_copy(held.at[index], target.at[rows, :], sems.at[index, which])
            copy.start()
            copies.append(copy)
    return copies


def join_kernel(*refs):
    packed, (qkv_hbm, proj_hbm, qkv_ref, proj_ref, sems) = refs[:-5], refs[-5:]
    copies = spread_quarters(packed, [0, 2], qkv_ref, proj_ref, qkv_hbm, proj_hbm, sems)
    for copy in copies:
        copy.wait()


def halve_kernel(keep_ref, got_ref, hold_ref, send_ref):
    total = keep_ref[...].astype(jnp.float32) + got_ref[...].astype(jnp.float32)
    rows = hold_ref.shape[0]
    hold_ref[...] = total[0:rows]
    send_ref[0:rows, :] = total[rows:].astype(jnp.bfloat16)


def halve_both_kernel(
    keep_ref, got_ref, keep_two_ref, got_two_ref, hold_ref, send_ref, hold_two_ref
):
    rows = hold_ref.shape[0]
    halve_kernel(keep_ref, got_ref, hold_ref, send_ref)
    halve_kernel(keep_two_ref, got_two_ref, hold_two_ref, send_ref.at[rows : 2 * rows, :])


def last_kernel(
    chip_ref,
    both_a_ref,
    both_b_ref,
    old_qkv,
    old_proj,
    qkv_hbm,
    proj_hbm,
    qkv_ref,
    proj_ref,
    sems,
):
    copies = []
    rows = both_a_ref.shape[0]
    inner = qkv_ref.shape[2]
    chips = (chip_ref.at[0:rows, :], chip_ref.at[rows : 2 * rows, :])
    for index, piece_ref in enumerate((*chips, both_a_ref, both_b_ref)):
        start = ((own_quarter() ^ (1 if index < 2 else 3)) * 2 + index % 2) * rows
        target = pl.ds(pl.multiple_of(start, rows), rows)
        qkv_ref[index] = piece_ref[:, 0:inner].astype(jnp.float32)
        proj_ref[index] = piece_ref[:, inner:].astype(jnp.float32)
        for which, (held, whole) in enumerate(((qkv_ref, qkv_hbm), (proj_ref, proj_hbm))):
            copy = pltpu.make_async_copy(held.at[index], whole.at[target, :], sems.at[index, which])
            copy.start()
            copies.append(copy)
    for copy in copies:
        copy.wait()


def sums_kernel(
    sums_ref,
    got_sums_ref,
    hold_one_ref,
    hold_two_ref,
    got_ref,
    share_ref,
    gains_ref,
    shifts_ref,
    conv_ref,
    qv_ref,
    bias_ref,
):
    rows = hold_one_ref.shape[0]
    for which, hold_ref in enumerate((hold_one_ref, hold_two_ref)):
        got = got_ref[which * rows : (which + 1) * rows, :].astype(jnp.float32)
        share_ref[which] = (hold_ref[...] + got).reshape(share_ref.shape[1:])
    total = sums_ref[...] + got_sums_ref[...]
    for row, start in enumerate((0, 2, 5)):
        gains_ref[row : row + 1, :] = total[start : start + 1]
        shifts_ref[row : row + 1, :] = total[start + 1 : start + 2]
    conv_ref[0:1, :] = total[4:5]
    conv_ref[1:2, :] = total[7:8]
    qv_ref[...] = total[8:10]
    bias_ref[...] = total[10:11]


def call_kernel(kernel, outputs, scratch, operands, places, flops, limit, out_places=None, aliases={}):
    out_places = out_places or "v" * len(outputs)
    spaces = {
        "v": pl.BlockSpec(memory_space=pltpu.VMEM),
        "s": pl.BlockSpec(memory_space=pltpu.SMEM),
        "h": pl.BlockSpec(memory_space=pl.ANY),
        "o": pl.BlockSpec(memory_space=pltpu.VMEM),
        "a": pl.BlockSpec(memory_space=pl.ANY),
    }
    moved = 8 * flops // LANES
    held = {"v": pltpu.VMEM, "h": pltpu.HBM, "o": jax.ShapeDtypeStruct}
    operands = [
        pltpu.with_memory_space_constraint(array, pltpu.HBM) if place == "h" else array
        for array, place in zip(operands, places)
    ]
    return pl.pallas_call(
        kernel,
        out_shape=[held[place](*output) for output, place in zip(outputs, out_places)],
        in_specs=[spaces[place] for place in places],
        out_specs=[spaces[place] for place in out_places],
        scratch_shapes=scratch,
        input_output_aliases=aliases,
        compiler_params=pltpu.CompilerParams(vmem_limit_bytes=limit * 2**20),
        cost_estimate=pl.CostEstimate(flops=flops, bytes_accessed=moved, transcendentals=0),
    )(*operands)


def send_height(block, step):
    size = lax.axis_size("height")
    return lax.ppermute(block, "height", [(i, i ^ step) for i in range(size)])


def with_cores(blocks, other):
    pieces = [blocks[0], other]
    for block in blocks[1:]:
        pieces += [block, send_height(block, 1)]
    return pieces


def send_canvas(block, step):
    size = lax.axis_size("canvas")
    return lax.ppermute(block, "canvas", [(i, i ^ step) for i in range(size)])


def send_phase(block, phase):
    canvases, size = lax.axis_size("canvas"), lax.axis_size("height")
    pairs = []
    for canvas in range(canvases):
        for height in range(size):
            step = 2 if (height ^ phase) & 1 else 1
            pairs.append((canvas * size + height, (canvas ^ step) * size + height))
    return lax.ppermute(block, ("canvas", "height"), pairs)


def trade_canvas(pieces):
    return [pieces[0]] + [send_canvas(piece, step) for step, piece in enumerate(pieces) if step]


def whole_canvas(
    features,
    tile_ids,
    norm_gains,
    norm_shifts,
    conv_weights,
    conv_biases,
    qkv_weight,
    qv_bias,
    proj_weight,
    proj_bias,
    cotangent,
):
    height_size = lax.axis_size("height")
    canvas_size = lax.axis_size("canvas")
    local_rows, cols, channels = features.shape[1:]
    all_rows = tile_ids.shape[1]
    pixels = all_rows * cols
    own_pixels = local_rows * cols
    out_share = channels // height_size
    ci_share = channels // canvas_size
    quarter = channels // 4
    row_share = quarter // canvas_size
    low, wide = jnp.bfloat16, jnp.float32

    own_features = features.reshape(own_pixels, channels)
    own_grad = cotangent.reshape(own_pixels, channels)
    steps = range(2, height_size, 2)
    held_features = [own_features] + [send_height(own_features, step) for step in steps]
    plane = ((pixels, channels), low)
    plane_wide = ((pixels, channels), wide)
    sums_shape = ((16, channels), wide)
    mixed_shapes = [((row_share, 4 * channels), low)] * canvas_size
    taps = pltpu.VMEM((pixels + 2 * cols, 3 * channels), low)
    held_wide = pltpu.VMEM((pixels, channels), wide)
    flipped = pltpu.VMEM((channels, pixels), low)
    narrow = pltpu.VMEM((NARROW, pixels), low)
    columns = pltpu.VMEM((9 * out_share, pixels), low)
    part_held = pltpu.VMEM((9 * out_share, channels), low)
    sem = pltpu.SemaphoreType.DMA
    conv_flops = 2 * 9 * pixels * channels * channels
    dot_flops = 2 * pixels * channels * channels
    score_flops = 2 * pixels * pixels * channels
    scale = channels ** (-0.5)

    (
        held_conv,
        turned,
        held_qkv,
        held_proj,
        params,
        mask,
        lane_mask,
        id_rows,
        id_cols,
    ) = call_kernel(
        functools.partial(hold_kernel, cols=cols),
        [
            (conv_weights.shape, low),
            ((2, 3, channels, 3 * channels), low),
            (qkv_weight.shape, low),
            (proj_weight.shape, low),
            ((24, channels), wide),
            ((2, pixels, LANES), wide),
            ((8, pixels), wide),
            ((pixels, LANES), jnp.int32),
            ((8, pixels), jnp.int32),
        ],
        [
            pltpu.SMEM(tile_ids.shape, jnp.int32),
            pltpu.VMEM(norm_gains.shape, wide),
            pltpu.VMEM(norm_shifts.shape, wide),
            pltpu.VMEM(conv_biases.shape, wide),
            pltpu.VMEM(qv_bias.shape, wide),
            pltpu.VMEM((1, channels), wide),
            sem((27,)),
        ],
        [
            tile_ids,
            norm_gains,
            norm_shifts,
            conv_biases,
            conv_weights,
            qkv_weight,
            proj_weight,
            qv_bias,
            proj_bias.reshape(1, channels),
        ],
        "h" * 9,
        conv_flops,
        8,
    )
    held_features[1:] = [
        lax.optimization_barrier((params, block))[1] for block in held_features[1:]
    ]
    other_core = send_height(jnp.concatenate([own_features, own_grad], axis=0), 1)
    pieces = with_cores(held_features, other_core)
    far_grad, *pieces[4::2] = lax.optimization_barrier((own_grad, *held_features[2:]))
    held_grads = [own_grad, send_height(own_grad, 2)]
    held_grads[1], pieces[2] = lax.optimization_barrier((held_grads[1], held_features[1]))
    held_grads += [send_height(far_grad, step) for step in steps[1:]]

    all_features, act_one, middle, act_two, residual, table = call_kernel(
        functools.partial(conv_kernel, cols=cols, count=height_size),
        [plane, plane, plane_wide, plane, plane_wide, ((24, channels), wide)],
        [pltpu.VMEM((own_pixels, channels), low), taps, sem],
        [*pieces, held_conv, params, mask],
        "h" + "v" * (height_size + 2),
        2 * conv_flops,
        16,
    )
    residual, *held_grads = lax.optimization_barrier((residual, *held_grads))
    grad_pieces = with_cores(held_grads, other_core)
    normed, query, key, value, soft, out_flip, output = call_kernel(
        functools.partial(score_kernel, score_scale=scale),
        [
            plane,
            plane,
            plane,
            plane,
            ((pixels, pixels), low),
            ((channels, pixels), low),
            ((own_pixels, channels), low),
        ],
        [
            flipped,
            *[pltpu.VMEM((pixels, SCORE_ROWS), wide)] * (pixels // SCORE_ROWS),
        ],
        [
            held_qkv,
            held_proj,
            residual,
            table,
            id_rows,
            id_cols,
        ],
        "vvvvvv",
        3 * dot_flops + 2 * score_flops,
        20,
        "v" * 6 + "o",
    )
    normed, *grad_pieces = lax.optimization_barrier((normed, *grad_pieces))
    all_grad, packed, sums, *mixed = call_kernel(
        functools.partial(attention_kernel, score_scale=scale, count=height_size),
        [plane, ((pixels, 3 * channels), low), sums_shape, *mixed_shapes],
        [
            pltpu.VMEM((quarter, 4 * channels), low),
            flipped,
            pltpu.VMEM((pixels, channels), low),
            pltpu.VMEM((pixels, pixels), low),
            pltpu.VMEM((quarter, pixels), low),
            sem((height_size,)),
            *[pltpu.VMEM((pixels, SCORE_ROWS), wide)] * (pixels // SCORE_ROWS),
        ],
        [held_proj, normed, query, key, value, soft, out_flip, *grad_pieces],
        "vvvvvvvh" + "a" * (height_size - 1),
        3 * dot_flops + 4 * score_flops,
        20,
    )
    mixed = trade_canvas(mixed)
    total_three, scales_three, sums, part_two = call_kernel(
        functools.partial(third_kernel, cols=cols),
        [plane_wide, ((8, channels), wide), sums_shape, ((9 * out_share, channels), low)],
        [narrow, columns],
        [held_qkv, all_grad, packed, residual, table, act_two, lane_mask, sums],
        "vvvvvvvv",
        3 * dot_flops + conv_flops // height_size,
        16,
    )
    half_total, half_taps, sums = call_kernel(
        functools.partial(turn_kernel, cols=cols),
        [plane_wide, (taps.shape, low), sums_shape],
        [],
        [all_grad, total_three, scales_three, residual, mask, turned, sums],
        "vvvvvvv",
        conv_flops // 2,
        16,
    )
    half_total, *mixed = lax.optimization_barrier((half_total, *mixed))
    mixed_sum = mixed[0].astype(wide)
    for piece in mixed[1:]:
        mixed_sum = mixed_sum + piece.astype(wide)
    mixed_sum = mixed_sum.astype(low)
    joints = trade_canvas([mixed_sum] * canvas_size)
    halves = [((2 * 9 * out_share, ci_share), low)] * 4
    total_two, scales, sums, keep_one, send_one, keep_two, send_two = call_kernel(
        functools.partial(second_kernel, cols=cols),
        [plane_wide, ((8, channels), wide), sums_shape, *halves],
        [narrow, columns, part_held],
        [half_total, half_taps, middle, table, act_one, mask, lane_mask, turned, sums, part_two],
        "v" * 10,
        conv_flops // 2,
        20,
    )
    total_two, *joints = lax.optimization_barrier((total_two, *joints))
    (own_mixed,) = call_kernel(
        place_kernel,
        [((quarter, 4 * channels), low)],
        [],
        joints,
        "v" * canvas_size,
        1,
        12,
    )
    own_mixed, send_one, send_two = lax.optimization_barrier((own_mixed, send_one, send_two))
    chip_mixed = send_height(own_mixed, 2)
    core_mixed = send_height(own_mixed, 1)
    got_one, got_two = send_phase(send_one, 0), send_phase(send_two, 0)
    own_total, sums, partial_sums = call_kernel(
        functools.partial(first_kernel, cols=cols),
        [((own_pixels, channels), wide), sums_shape, sums_shape],
        [held_wide, taps],
        [total_two, scales, middle, all_features, table, mask, sums, turned],
        "vvvvvvvv",
        1,
        20,
    )
    got_sums, own_sums = send_phase(sums, 0), sums
    sums, core_mixed, got_one, got_two = lax.optimization_barrier(
        (sums, core_mixed, got_one, got_two)
    )
    share_rows = 9 * out_share
    hold_one, send_share, hold_two = call_kernel(
        halve_both_kernel,
        [
            ((share_rows, ci_share), wide),
            ((2 * share_rows, ci_share), low),
            ((share_rows, ci_share), wide),
        ],
        [],
        [keep_one, got_one, keep_two, got_two],
        "vvvv",
        1,
        12,
    )
    got_share = send_phase(send_share, 1)

    def widened(count, rows):
        return [
            pltpu.VMEM((count, rows, 3 * channels), wide),
            pltpu.VMEM((count, rows, channels), wide),
            sem((count, 2)),
        ]

    grad_shapes = [(qkv_weight.shape, wide), (proj_weight.shape, wide)]
    core_mixed, hold_one = lax.optimization_barrier((core_mixed, hold_one))
    qkv_grad, proj_grad = call_kernel(
        join_kernel,
        grad_shapes,
        widened(2, quarter),
        [own_mixed, core_mixed],
        "vv",
        1,
        12,
        "hh",
    )
    qkv_grad, chip_mixed, got_sums = lax.optimization_barrier((qkv_grad, chip_mixed, got_sums))
    sums = own_sums + got_sums
    got_sums = send_phase(sums, 1)
    chip_halves = call_kernel(
        cut_kernel,
        [((quarter // 2, 4 * channels), low)] * 2,
        [],
        [chip_mixed],
        "v",
        1,
        12,
    )
    both_halves = [send_height(half, 1) for half in chip_halves]
    qkv_grad, proj_grad = call_kernel(
        last_kernel,
        grad_shapes,
        widened(4, quarter // 2),
        [chip_mixed, *both_halves, qkv_grad, proj_grad],
        "vvvhh",
        1,
        12,
        "hh",
        {3: 0, 4: 1},
    )
    qkv_grad, own_total = lax.optimization_barrier((qkv_grad, own_total))
    (input_grad,) = call_kernel(
        own_kernel,
        [((own_pixels, channels), low)],
        [],
        [
            own_total,
            partial_sums,
            all_features,
            all_grad,
            total_three,
            residual,
            scales_three,
            table,
        ],
        "v" * 8,
        dot_flops // 4,
        12,
        "o",
    )
    input_grad, got_share, got_sums = lax.optimization_barrier((input_grad, got_share, got_sums))
    vector_shapes = [norm_gains.shape, norm_shifts.shape, conv_biases.shape, qv_bias.shape]
    conv_grad, gains_grad, shifts_grad, biases_grad, qv_grad, proj_bias_grad = call_kernel(
        sums_kernel,
        [((2, 3, 3, out_share, ci_share), wide)]
        + [(shape, wide) for shape in vector_shapes + [(1, channels)]],
        [],
        [sums, got_sums, hold_one, hold_two, got_share],
        "vvvvv",
        1,
        12,
        "o" * 6,
    )
    own_shape = (1, local_rows, cols, channels)
    return (
        output.reshape(own_shape),
        input_grad.reshape(own_shape),
        gains_grad,
        shifts_grad,
        jnp.swapaxes(conv_grad, 3, 4),
        biases_grad,
        qkv_grad,
        qv_grad,
        proj_grad,
        proj_bias_grad.reshape(channels),
    )


def on_device(*arrays):
    features, tile_ids = arrays[0], arrays[1]
    local_rows, cols, channels = features.shape[1:]
    pixels = tile_ids.shape[1] * cols
    height_size, canvas_size = lax.axis_size("height"), lax.axis_size("canvas")
    powers = all(size & (size - 1) == 0 for size in (height_size, canvas_size, cols))
    fits = (
        powers
        and height_size > 2
        and canvas_size == 4
        and channels == LANES * canvas_size
        and pixels <= MOST_PIXELS
        and pixels % FILL_ROWS == 0
        and pixels >= EARLY_ROWS
        and FILL_ROWS % CHUNK == 0
        and pixels % SCORE_ROWS == 0
        and pixels % KEY_ROWS == 0
        and (local_rows * cols) % LANES == 0
        and CHUNK % cols == 0
        and cols % 16 == 0
        and channels % (LANES * canvas_size) == 0
        and 2 * channels == NARROW * height_size
    )
    return whole_canvas(*arrays) if fits else split_canvas(*arrays)


def solution(mesh):
    in_specs = (
        P("canvas", "height", None, None),
        P("canvas", None),
        P(),
        P(),
        P(),
        P(),
        P(),
        P(),
        P(),
        P(),
        P("canvas", "height", None, None),
    )
    out_specs = (
        P("canvas", "height", None, None),
        P("canvas", "height", None, None),
        P(),
        P(),
        P(None, None, None, "canvas", "height"),
        P(),
        P(),
        P(),
        P(),
        P(),
    )
    return jax.shard_map(
        on_device, mesh=mesh, in_specs=in_specs, out_specs=out_specs, check_vma=False
    )
```

```python
import functools

import jax
import jax.numpy as jnp
from jax import lax
from jax.experimental import pallas as pl
from jax.experimental.pallas import tpu as pltpu
from jax.sharding import PartitionSpec as P

GROUPS = 32


epsilon = 1e-06
masked_score = -1e30
MOST_PIXELS = 1024
LANES = 128
NARROW = 128
CHUNK = 128
FILL_ROWS = 256
EARLY_ROWS = 512
SCORE_ROWS = 256
KEY_ROWS = 256


def extended(block, sides, width):
    for axis, dim in sides:
        count = lax.axis_size(axis)
        forward = [(i, i + 1) for i in range(count - 1)]
        backward = [(target, source) for source, target in forward]
        low = lax.ppermute(
            lax.slice_in_dim(block, block.shape[dim] - width, None, axis=dim), axis, forward
        )
        high = lax.ppermute(lax.slice_in_dim(block, 0, width, axis=dim), axis, backward)
        block = jnp.concatenate([low, block, high], axis=dim)
    return block


def group_total(vector):
    return vector.reshape(GROUPS, -1).sum(axis=1)


def spread_groups(vector, channels):
    return jnp.repeat(vector, channels // GROUPS)


def norm_forward(values, gain, shift, members):
    channels = values.shape[1]
    totals = lax.psum(group_total(jnp.sum(values, axis=0)), "height")
    centered = values - spread_groups(totals / members, channels)
    squares = lax.psum(group_total(jnp.sum(centered * centered, axis=0)), "height")
    inverse = spread_groups(lax.rsqrt(squares / members + epsilon), channels)
    normed = centered * inverse
    return (normed, inverse, normed * gain + shift)


def norm_backward(grad_in, normed, inverse, gain, members):
    channels = grad_in.shape[1]
    scaled = grad_in * gain
    both_sums = lax.psum(
        (group_total(jnp.sum(scaled, axis=0)), group_total(jnp.sum(scaled * normed, axis=0))),
        "height",
    )
    mean_grad = spread_groups(both_sums[0] / members, channels)
    mean_cross = spread_groups(both_sums[1] / members, channels)
    result = inverse * (scaled - mean_grad - normed * mean_cross)
    return (result, jnp.sum(grad_in * normed, axis=0), jnp.sum(grad_in, axis=0))


def swish(values):
    return values * jax.nn.sigmoid(values)


def swish_slope(values):
    sigmoid_part = jax.nn.sigmoid(values)
    return sigmoid_part * (1.0 + values * (1.0 - sigmoid_part))


def tap_columns(padded, row_mask, local_rows, canvas_cols):
    pieces = []
    for row_tap in range(3):
        rows_taken = padded[row_tap : row_tap + local_rows] * row_mask[:, row_tap, None, None]
        for col_tap in range(3):
            pieces.append(rows_taken[:, col_tap : col_tap + canvas_cols])
    stacked = jnp.concatenate(pieces, axis=2)
    return stacked.reshape(local_rows * canvas_cols, stacked.shape[2])


def conv_forward(acts, row_mask, weight, bias):
    local_rows, canvas_cols, channels = acts.shape
    rimmed = extended(acts, (("height", 0),), 1)
    padded = jnp.pad(rimmed, ((0, 0), (1, 1), (0, 0)))
    gathered = tap_columns(padded, row_mask, local_rows, canvas_cols)
    result = (
        jnp.dot(
            gathered, weight.reshape(9 * channels, channels), preferred_element_type=jnp.float32
        )
        + bias
    )
    return (result, gathered)


def conv_backward(grad_low, row_mask, weight, gathered):
    local_rows, canvas_cols, channels = grad_low.shape
    flat_grad = grad_low.reshape(local_rows * canvas_cols, channels)
    weight_grad = lax.dot_general(
        gathered, flat_grad, (((0,), (0,)), ((), ())), preferred_element_type=jnp.float32
    )
    rimmed = extended(grad_low, (("height", 0),), 1)
    padded = jnp.pad(rimmed, ((0, 0), (1, 1), (0, 0)))
    grad_taps = tap_columns(padded, row_mask, local_rows, canvas_cols)
    flipped = jnp.transpose(weight[::-1, ::-1], (0, 1, 3, 2)).reshape(9 * channels, channels)
    input_part = jnp.dot(grad_taps, flipped, preferred_element_type=jnp.float32)
    return (
        input_part,
        weight_grad.reshape(3, 3, channels, channels),
        jnp.sum(flat_grad.astype(jnp.float32), axis=0),
    )


def take_rows(array, offset, count):
    return lax.dynamic_slice_in_dim(array, offset, count)


def score_grads(
    queries, out_grad, log_total, row_dots, query_ids, key_rows, value_rows, key_ids, score_scale
):
    scores = (
        lax.dot_general(
            queries, key_rows, (((1,), (1,)), ((), ())), preferred_element_type=jnp.float32
        )
        * score_scale
    )
    same_tile = query_ids[:, None] == key_ids[None, :]
    softmax_block = jnp.exp(jnp.where(same_tile, scores - log_total[:, None], masked_score))
    weight_grad = lax.dot_general(
        out_grad, value_rows, (((1,), (1,)), ((), ())), preferred_element_type=jnp.float32
    )
    score_grad = (softmax_block * (weight_grad - row_dots[:, None])).astype(jnp.bfloat16)
    return (softmax_block.astype(jnp.bfloat16), score_grad)


def split_canvas(
    features,
    tile_ids,
    norm_gains,
    norm_shifts,
    conv_weights,
    conv_biases,
    qkv_weight,
    qv_bias,
    proj_weight,
    proj_bias,
    cotangent,
):
    height_size = lax.axis_size("height")
    local_rows = features.shape[1]
    canvas_cols = features.shape[2]
    channels = features.shape[3]
    pixels = local_rows * canvas_cols
    row_ids = tile_ids[0]
    all_rows = row_ids.shape[0]
    members = float(all_rows * canvas_cols * (channels // GROUPS))
    score_scale = channels ** (-0.5)
    first_row = lax.axis_index("height") * local_rows
    edge_ids = jnp.full((1,), -1, jnp.int32)
    padded_ids = jnp.concatenate([edge_ids, row_ids, edge_ids])
    near_ids = lax.dynamic_slice_in_dim(padded_ids, first_row, local_rows + 2)
    own_rows = near_ids[1 : local_rows + 1]
    row_mask = jnp.stack(
        [near_ids[row_tap : row_tap + local_rows] == own_rows for row_tap in range(3)], axis=1
    ).astype(jnp.bfloat16)
    key_ids = jnp.repeat(row_ids, canvas_cols)
    query_ids = jnp.repeat(own_rows, canvas_cols)
    grid_shape = (local_rows, canvas_cols, channels)
    inputs = features[0].reshape(pixels, channels).astype(jnp.float32)
    normed_one, inverse_one, pre_one = norm_forward(inputs, norm_gains[0], norm_shifts[0], members)
    act_one = swish(pre_one).astype(jnp.bfloat16).reshape(grid_shape)
    middle, taps_one = conv_forward(act_one, row_mask, conv_weights[0], conv_biases[0])
    normed_two, inverse_two, pre_two = norm_forward(middle, norm_gains[1], norm_shifts[1], members)
    act_two = swish(pre_two).astype(jnp.bfloat16).reshape(grid_shape)
    branch, taps_two = conv_forward(act_two, row_mask, conv_weights[1], conv_biases[1])
    residual = inputs + branch
    normed_three, inverse_three, pre_three = norm_forward(
        residual, norm_gains[2], norm_shifts[2], members
    )
    attn_input = pre_three.astype(jnp.bfloat16)
    mixed = jnp.dot(attn_input, qkv_weight, preferred_element_type=jnp.float32)
    queries = (mixed[:, :channels] + qv_bias[0]).astype(jnp.bfloat16)
    key_rows = mixed[:, channels : 2 * channels].astype(jnp.bfloat16)
    value_rows = (mixed[:, 2 * channels :] + qv_bias[1]).astype(jnp.bfloat16)
    running_max = jnp.full((pixels,), masked_score, jnp.float32)
    key_piece = lax.all_gather(key_rows, "height", axis=0, tiled=True)
    value_piece = lax.all_gather(value_rows, "height", axis=0, tiled=True)
    scores = (
        lax.dot_general(
            queries, key_piece, (((1,), (1,)), ((), ())), preferred_element_type=jnp.float32
        )
        * score_scale
    )
    same_tile = query_ids[:, None] == key_ids[None, :]
    scores = jnp.where(same_tile, scores, masked_score)
    new_max = jnp.maximum(running_max, jnp.max(scores, axis=1))
    weights = jnp.where(same_tile, jnp.exp(scores - new_max[:, None]), 0.0)
    summed_out = jnp.dot(
        weights.astype(jnp.bfloat16), value_piece, preferred_element_type=jnp.float32
    )
    total_weight = jnp.sum(weights, axis=1)
    log_total = new_max + jnp.log(total_weight)
    attended = summed_out / total_weight[:, None]
    attended_low = attended.astype(jnp.bfloat16)
    output = (
        residual
        + jnp.dot(attended_low, proj_weight, preferred_element_type=jnp.float32)
        + proj_bias
    )
    out_grad = cotangent[0].reshape(pixels, channels)
    out_grad_full = out_grad.astype(jnp.float32)
    proj_grad = lax.dot_general(
        attended_low, out_grad, (((0,), (0,)), ((), ())), preferred_element_type=jnp.float32
    )
    proj_bias_grad = jnp.sum(out_grad_full, axis=0)
    attended_grad = lax.dot_general(
        out_grad, proj_weight, (((1,), (1,)), ((), ())), preferred_element_type=jnp.float32
    ).astype(jnp.bfloat16)
    row_dots = jnp.sum(attended_grad.astype(jnp.float32) * attended, axis=1)
    block_rows = pixels * min(height_size, 8)
    zero_block = jnp.zeros((pixels, channels), jnp.float32)
    key_all, value_all = (
        lax.all_gather(key_rows, "height", axis=0, tiled=True),
        lax.all_gather(value_rows, "height", axis=0, tiled=True),
    )
    query_all, grad_all = (
        lax.all_gather(queries, "height", axis=0, tiled=True),
        lax.all_gather(attended_grad, "height", axis=0, tiled=True),
    )
    total_all, dots_all = (
        lax.all_gather(log_total, "height", axis=0, tiled=True),
        lax.all_gather(row_dots, "height", axis=0, tiled=True),
    )

    def own_query_step(running, block_index):
        offset = block_index * block_rows
        key_part = take_rows(key_all, offset, block_rows)
        rounded, score_grad = score_grads(
            queries,
            attended_grad,
            log_total,
            row_dots,
            query_ids,
            key_part,
            take_rows(value_all, offset, block_rows),
            take_rows(key_ids, offset, block_rows),
            score_scale,
        )
        return (
            running
            + jnp.dot(score_grad, key_part, preferred_element_type=jnp.float32) * score_scale,
            None,
        )

    def own_key_step(running, block_index):
        offset = block_index * block_rows
        query_part = take_rows(query_all, offset, block_rows)
        grad_part = take_rows(grad_all, offset, block_rows)
        rounded, score_grad = score_grads(
            query_part,
            grad_part,
            take_rows(total_all, offset, block_rows),
            take_rows(dots_all, offset, block_rows),
            take_rows(key_ids, offset, block_rows),
            key_rows,
            value_rows,
            query_ids,
            score_scale,
        )
        key_part = (
            lax.dot_general(
                score_grad, query_part, (((0,), (0,)), ((), ())), preferred_element_type=jnp.float32
            )
            * score_scale
        )
        value_part = lax.dot_general(
            rounded, grad_part, (((0,), (0,)), ((), ())), preferred_element_type=jnp.float32
        )
        return ((running[0] + key_part, running[1] + value_part), None)

    block_count = key_all.shape[0] // block_rows
    query_grad, unused_one = lax.scan(own_query_step, zero_block, jnp.arange(block_count))
    (key_grad, value_grad), unused_two = lax.scan(
        own_key_step, (zero_block, zero_block), jnp.arange(block_count)
    )
    query_low = query_grad.astype(jnp.bfloat16)
    key_low = key_grad.astype(jnp.bfloat16)
    value_low = value_grad.astype(jnp.bfloat16)
    stacked_grad = jnp.concatenate([query_low, key_low, value_low], axis=1)
    qkv_grad = lax.dot_general(
        attn_input, stacked_grad, (((0,), (0,)), ((), ())), preferred_element_type=jnp.float32
    )
    qv_grad = jnp.stack(
        [
            jnp.sum(query_low.astype(jnp.float32), axis=0),
            jnp.sum(value_low.astype(jnp.float32), axis=0),
        ]
    )
    normed_grad = lax.dot_general(
        stacked_grad, qkv_weight, (((1,), (1,)), ((), ())), preferred_element_type=jnp.float32
    )
    back_three, gain_three, shift_three = norm_backward(
        normed_grad, normed_three, inverse_three, norm_gains[2], members
    )
    residual_grad = out_grad_full + back_three
    grad_two = residual_grad.astype(jnp.bfloat16).reshape(grid_shape)
    act_two_grad, weight_two_grad, bias_two_grad = conv_backward(
        grad_two, row_mask, conv_weights[1], taps_two
    )
    middle_grad, gain_two, shift_two = norm_backward(
        act_two_grad * swish_slope(pre_two), normed_two, inverse_two, norm_gains[1], members
    )
    grad_one = middle_grad.astype(jnp.bfloat16).reshape(grid_shape)
    act_one_grad, weight_one_grad, bias_one_grad = conv_backward(
        grad_one, row_mask, conv_weights[0], taps_one
    )
    input_back, gain_one, shift_one = norm_backward(
        act_one_grad * swish_slope(pre_one), normed_one, inverse_one, norm_gains[0], members
    )
    input_grad = residual_grad + input_back
    conv_grad = jnp.stack([weight_one_grad, weight_two_grad])
    conv_part = lax.psum_scatter(conv_grad, "height", scatter_dimension=4, tiled=True)
    conv_part = lax.psum_scatter(
        conv_part.astype(jnp.bfloat16), "canvas", scatter_dimension=3, tiled=True
    ).astype(jnp.float32)
    summed = lax.psum(
        (
            jnp.stack([gain_one, gain_two, gain_three]),
            jnp.stack([shift_one, shift_two, shift_three]),
            jnp.stack([bias_one_grad, bias_two_grad]),
            qkv_grad,
            qv_grad,
            proj_grad,
            proj_bias_grad,
        ),
        ("canvas", "height"),
    )
    return (
        output.astype(jnp.bfloat16).reshape((1,) + grid_shape),
        input_grad.astype(jnp.bfloat16).reshape((1,) + grid_shape),
        summed[0],
        summed[1],
        conv_part,
        summed[2],
        summed[3],
        summed[4],
        summed[5],
        summed[6],
    )


def fold(block):
    rows, width = block.shape
    return jnp.sum(block.reshape(rows // 8, 8, width), axis=0)


def group_lanes(block, group):
    lane = lax.broadcasted_iota(jnp.int32, block.shape, 1)
    width = block.shape[1]
    step = 1
    while step < group:
        above = pltpu.roll(block, step, 1)
        below = pltpu.roll(block, width - step, 1)
        block = block + jnp.where((lane & step) != 0, above, below)
        step *= 2
    return block


def group_mean(partial, members):
    spread = group_lanes(partial, partial.shape[1] // GROUPS)
    return jnp.sum(spread, axis=0, keepdims=True) * (1.0 / members)


def widen(block, width):
    return jnp.concatenate([block] * (width // block.shape[1]), axis=1)


def each_block(pixels, block, body, carry=0):
    def step(index, carry):
        return body(pl.ds(pl.multiple_of(index * block, block), block), carry)

    return lax.fori_loop(0, pixels // block, step, carry)


def each_chunk(pixels, body, carry):
    return each_block(pixels, CHUNK, body, carry)


def aligned(start, step):
    return start if isinstance(start, int) else pl.multiple_of(start, step)


class RunningStats:
    def __init__(self, channels):
        self.width = channels // GROUPS
        self.reference = None
        self.sums = self.squares = jnp.zeros((8, channels), jnp.float32)

    def add(self, block):
        if self.reference is None:
            self.reference = group_mean(block[0:8], 8.0 * self.width)
        offset = block - self.reference
        self.sums = self.sums + fold(offset)
        self.squares = self.squares + fold(offset * offset)

    def finish(self, pixels):
        both = group_lanes(jnp.concatenate([self.sums, self.squares], axis=0), self.width)
        share = 1.0 / (pixels * self.width)
        offset = column_total(both[0:8]) * share
        variance = column_total(both[8:16]) * share - offset * offset
        return self.reference + offset, lax.rsqrt(jnp.maximum(variance, 0.0) + epsilon)


def put_taps(taps_ref, block, rows, cols):
    count, channels = block.shape
    place = lax.broadcasted_iota(jnp.int32, block.shape, 0) & (cols - 1)
    left = jnp.where(place == 0, 0.0, pltpu.roll(block, 1, 0))
    right = jnp.where(place == cols - 1, 0.0, pltpu.roll(block, count - 1, 0))
    inner = pl.ds(aligned(rows.start + cols, cols), count)
    taps_ref[inner, 0:channels] = left.astype(jnp.bfloat16)
    taps_ref[inner, channels : 2 * channels] = block.astype(jnp.bfloat16)
    taps_ref[inner, 2 * channels :] = right.astype(jnp.bfloat16)


def clear_edges(taps_ref, cols):
    edge = jnp.zeros((cols, taps_ref.shape[1]), taps_ref.dtype)
    taps_ref[0:cols, :] = edge
    taps_ref[taps_ref.shape[0] - cols :, :] = edge


def begin_conv(taps_ref, product, total_ref, fill, first, cols):
    for start in range(0, total_ref.shape[0], FILL_ROWS):
        for inner in range(start, start + FILL_ROWS, CHUNK):
            fill(pl.ds(inner, CHUNK))
        rows = pl.ds(start, FILL_ROWS)
        total_ref[rows, :] = first(rows, product(taps_ref, pl.ds(start + cols, FILL_ROWS), 1))


def add_rows(taps_ref, product, mask_ref, total_ref, stop, cols):
    rows = pl.ds(0, stop)
    part = product(taps_ref, rows, 0)
    total_ref[rows, :] += widen(mask_ref[0, rows, :], total_ref.shape[1]) * part


def end_conv(taps_ref, product, mask_ref, total_ref, last, cols, old_ref=None, pending=None):
    pixels, channels = total_ref.shape
    old_ref = total_ref if old_ref is None else old_ref
    pending = pixels if pending is None else pending
    for start in range(0, pixels, FILL_ROWS):
        rows = pl.ds(start, FILL_ROWS)
        value = old_ref[rows, :]
        for row_tap in (0, 2) if start >= pending else (2,):
            part = product(taps_ref, pl.ds(start + row_tap * cols, FILL_ROWS), row_tap)
            value = value + widen(mask_ref[row_tap // 2, rows, :], channels) * part
        total_ref[rows, :] = last(rows, value)


def run_conv(taps_ref, product, mask_ref, total_ref, fill, first, last, cols):
    begin_conv(taps_ref, product, total_ref, fill, first, cols)
    add_rows(taps_ref, product, mask_ref, total_ref, total_ref.shape[0], cols)
    end_conv(taps_ref, product, mask_ref, total_ref, last, cols)


def product_forward(weight_ref):
    channels = weight_ref.shape[-1]

    def product(taps_ref, shifted, row_tap):
        return jnp.dot(
            taps_ref[shifted, :],
            weight_ref[row_tap].reshape(3 * channels, channels),
            preferred_element_type=jnp.float32,
        )

    return product


def product_backward(weight_ref):
    def product(taps_ref, shifted, row_tap):
        return lax.dot_general(
            taps_ref[shifted, :],
            weight_ref[row_tap],
            (((1,), (1,)), ((), ())),
            preferred_element_type=jnp.float32,
        )

    return product


def activation(read, mean, inverse, gain, shift, act_ref, taps_ref, cols):
    scale, offset = 0.5 * inverse * gain, 0.5 * shift

    def fill(rows):
        half = (read(rows) - mean) * scale + offset
        act = half * (1.0 + jnp.tanh(half))
        act_ref[rows, :] = act.astype(jnp.bfloat16)
        put_taps(taps_ref, act, rows, cols)

    return fill


def back_means(sums, gain, pixels):
    channels = gain.shape[1]
    members = float(pixels * (channels // GROUPS))
    return group_mean(sums[0] * gain, members), group_mean(sums[1] * gain, members)


def column_total(partial):
    return jnp.sum(partial, axis=0, keepdims=True)


def weight_part(act_ref, narrow, lanes_ref, flip_ref, columns_ref, part_ref, cols):
    pixels, channels = act_ref.shape
    height = lax.axis_index("height")
    share = NARROW // 2
    flip_ref[...] = narrow.T
    own = pl.ds(pl.multiple_of((height % 2) * share, share), share)
    grad = flip_ref[own, :].astype(jnp.float32)
    column = lax.broadcasted_iota(jnp.int32, grad.shape, 1) & (cols - 1)
    for col_tap in range(3):
        shifted = grad
        if col_tap == 0:
            shifted = jnp.where(column == cols - 1, 0.0, pltpu.roll(grad, pixels - 1, 1))
        elif col_tap == 2:
            shifted = jnp.where(column == 0, 0.0, pltpu.roll(grad, 1, 1))
        for row_tap in range(3):
            tap = 3 * row_tap + col_tap
            place = slice(tap * share, (tap + 1) * share)
            if row_tap == 1:
                columns_ref[place, :] = shifted.astype(jnp.bfloat16)
                continue
            side, turn = (0, pixels - cols) if row_tap == 0 else (1, cols)
            masked = (shifted * lanes_ref[side : side + 1, :]).astype(jnp.bfloat16)
            columns_ref[place, :] = pltpu.roll(masked, turn, 1)
    part_ref[...] = jnp.dot(
        columns_ref[...], act_ref[...], preferred_element_type=jnp.float32
    ).astype(jnp.bfloat16)


def begin_back(read, weights_ref, mask_ref, taps_ref, total_ref, stop, cols):
    clear_edges(taps_ref, cols)

    def fill(rows):
        put_taps(taps_ref, read(rows), rows, cols)

    product = product_backward(weights_ref)
    begin_conv(taps_ref, product, total_ref, fill, lambda rows, part: part, cols)
    if stop:
        add_rows(taps_ref, product, mask_ref, total_ref, stop, cols)


def finish_back(
    weights_ref,
    mask_ref,
    taps_ref,
    total_ref,
    read,
    table_ref,
    which,
    cols,
    old_ref=None,
    pending=None,
):
    mean, inverse, gain, shift = norm_rows(table_ref, which)
    scale, offset = 0.5 * inverse * gain, 0.5 * shift
    sums = []

    def slope(rows, value):
        centered = read(rows) - mean
        half = centered * scale + offset
        turn = jnp.tanh(half)
        double = value * ((1.0 + turn) * (1.0 + half * (1.0 - turn)))
        sums.append((fold(double), fold(double * centered)))
        return double

    product = product_backward(weights_ref)
    end_conv(taps_ref, product, mask_ref, total_ref, slope, cols, old_ref, pending)
    plain, cross = sum(pair[0] for pair in sums), sum(pair[1] for pair in sums)
    return 0.5 * plain, 0.5 * inverse * cross


def norm_back(total_ref, double, sums, read, table_ref, which, pixels, scales_ref=None):
    mean, inverse, gain, shift = norm_rows(table_ref, which)
    mean_grad, mean_cross = back_means(sums, gain, pixels)
    slope = inverse * gain * (0.5 if double else 1.0)
    level, tilt = inverse * mean_grad, inverse * inverse * mean_cross
    if scales_ref is not None:
        for row, scales in enumerate((mean, slope, level, tilt)):
            scales_ref[row : row + 1, :] = scales

    def back(rows, inner):
        return total_ref[inner, :] * slope - level - (read(rows) - mean) * tilt

    return back


def own_lanes():
    block = lax.axis_index("height") // 2
    return pl.ds(pl.multiple_of(block * NARROW, NARROW), NARROW)


def narrow_back(total_ref, value_ref, scales_ref):
    lanes = own_lanes()
    mean, slope, level, tilt = (scales_ref[row : row + 1, lanes] for row in range(4))
    return total_ref[:, lanes] * slope - level - (value_ref[:, lanes] - mean) * tilt


def scaled_back(total_ref, value_ref, scales_ref, rows, inner):
    mean, slope, level, tilt = (scales_ref[row : row + 1, :] for row in range(4))
    return total_ref[inner, :] * slope - level - (value_ref[rows, :].astype(jnp.float32) - mean) * tilt


def turn_kernel(
    grad_ref,
    total_three_ref,
    scales_ref,
    residual_ref,
    mask_ref,
    weights_ref,
    old_sums_ref,
    total_ref,
    taps_ref,
    sums_ref,
    *,
    cols,
):
    grad_sums = []

    def read(rows):
        grad = scaled_back(total_three_ref, residual_ref, scales_ref, rows, rows)
        grad = grad_ref[rows, :].astype(jnp.float32) + grad
        grad = grad.astype(jnp.bfloat16).astype(jnp.float32)
        grad_sums.append(fold(grad))
        return grad

    begin_back(read, weights_ref.at[1], mask_ref, taps_ref, total_ref, EARLY_ROWS, cols)
    sums_ref[...] = old_sums_ref[...]
    sums_ref[7:8, :] = column_total(sum(grad_sums))


def norm_rows(table_ref, which):
    picks = (2 * which, 2 * which + 1, 6 + which, 9 + which)
    return tuple(table_ref[pick : pick + 1, :] for pick in picks)


def build_masks(ids_ref, mask_ref, lanes_ref, id_rows_ref, id_cols_ref, cols):
    rows = ids_ref.shape[1]

    def one_row(row, carry):
        here = ids_ref[0, row]
        place = pl.ds(pl.multiple_of(row * cols, cols), cols)
        id_rows_ref[place, :] = jnp.full((cols, LANES), here, jnp.int32)
        for side, other in ((0, row - 1), (1, row + 1)):
            inside = jnp.logical_and(other >= 0, other < rows)
            other_id = ids_ref[0, jnp.clip(other, 0, rows - 1)]
            same = jnp.where(jnp.logical_and(inside, other_id == here), 1.0, 0.0)
            mask_ref[side, place, :] = jnp.full((cols, LANES), same, jnp.float32)
        return carry

    lax.fori_loop(0, rows, one_row, 0)
    lane = lax.broadcasted_iota(jnp.int32, (8, LANES), 1)
    each = LANES // cols
    for block in range(rows // each):
        ids = jnp.full((8, LANES), ids_ref[0, block * each], jnp.int32)
        for step in range(1, each):
            ids = jnp.where(lane >= step * cols, ids_ref[0, block * each + step], ids)
        id_cols_ref[:, block * LANES : (block + 1) * LANES] = ids
    ids = id_cols_ref[...].astype(jnp.float32)
    pixels = ids.shape[1]
    pixel = lax.broadcasted_iota(jnp.int32, ids.shape, 1)
    above = jnp.where(pixel < cols, -1.0, pltpu.roll(ids, cols, 1))
    below = jnp.where(pixel >= pixels - cols, -1.0, pltpu.roll(ids, pixels - cols, 1))
    lanes_ref[0:1, :] = jnp.where(above == ids, 1.0, 0.0)[0:1]
    lanes_ref[1:2, :] = jnp.where(below == ids, 1.0, 0.0)[0:1]


def hold_kernel(
    ids_hbm,
    gains_hbm,
    shifts_hbm,
    biases_hbm,
    weights_hbm,
    qkv_hbm,
    proj_hbm,
    qv_bias_hbm,
    proj_bias_hbm,
    weights_ref,
    turned_ref,
    qkv_ref,
    proj_ref,
    table_ref,
    mask_ref,
    lanes_ref,
    id_rows_ref,
    id_cols_ref,
    ids_ref,
    gains_ref,
    shifts_ref,
    biases_ref,
    qv_bias_ref,
    proj_bias_ref,
    sems,
    *,
    cols,
):
    channels = weights_ref.shape[-1]
    small = [
        (ids_hbm, ids_ref),
        (gains_hbm, gains_ref),
        (shifts_hbm, shifts_ref),
        (biases_hbm, biases_ref),
        (qv_bias_hbm, qv_bias_ref),
        (proj_bias_hbm, proj_bias_ref),
    ]
    large = [(weights_hbm, weights_ref), (qkv_hbm, qkv_ref), (proj_hbm, proj_ref)]
    for which in range(2):
        for row_tap in range(3):
            for col_tap in range(3):
                place = slice(col_tap * channels, (col_tap + 1) * channels)
                large.append(
                    (
                        weights_hbm.at[which, 2 - row_tap, 2 - col_tap],
                        turned_ref.at[which, row_tap, :, place],
                    )
                )
    copies = [
        pltpu.make_async_copy(source, target, sems.at[index])
        for index, (source, target) in enumerate(small + large)
    ]
    for copy in copies:
        copy.start()
    for copy in copies[: len(small)]:
        copy.wait()
    build_masks(ids_ref, mask_ref, lanes_ref, id_rows_ref, id_cols_ref, cols)
    table_ref[6:9, :] = gains_ref[...]
    table_ref[9:12, :] = shifts_ref[...]
    table_ref[12:14, :] = biases_ref[...]
    table_ref[14:16, :] = qv_bias_ref[...]
    table_ref[16:17, :] = proj_bias_ref[...]
    for copy in copies[len(small) :]:
        copy.wait()


def conv_kernel(*refs, cols, count):
    pieces, refs = refs[:count], refs[count:]
    (
        weights_ref,
        params_ref,
        mask_ref,
        features_ref,
        act_one_ref,
        middle_ref,
        act_two_ref,
        residual_ref,
        table_ref,
        own_ref,
        taps_ref,
        sem,
    ) = refs
    pixels, channels = features_ref.shape
    wide = jnp.float32
    own_copy = pltpu.make_async_copy(pieces[0], own_ref, sem)
    own_copy.start()
    table_ref[...] = params_ref[...]
    clear_edges(taps_ref, cols)

    def read_input(rows):
        return features_ref[rows, :].astype(wide)

    def read_middle(rows):
        return middle_ref[rows, :]

    height = lax.axis_index("height")
    own_pixels = pixels // count
    seen = RunningStats(channels)
    for place in list(range(1, count)) + [0]:
        if place == 0:
            own_copy.wait()
        piece = (pieces[place] if place else own_ref)[0:own_pixels, :]
        start = pl.multiple_of((height ^ place) * own_pixels, own_pixels)
        features_ref[pl.ds(start, own_pixels), :] = piece
        seen.add(piece.astype(wide))
    table_ref[0:1, :], table_ref[1:2, :] = seen.finish(pixels)
    seen = RunningStats(channels)

    def keep(rows, value):
        seen.add(value)
        return value

    run_conv(
        taps_ref,
        product_forward(weights_ref.at[0]),
        mask_ref,
        middle_ref,
        activation(read_input, *norm_rows(table_ref, 0), act_one_ref, taps_ref, cols),
        lambda rows, part: part + table_ref[12:13, :],
        keep,
        cols,
    )
    table_ref[2:3, :], table_ref[3:4, :] = seen.finish(pixels)
    seen = RunningStats(channels)
    run_conv(
        taps_ref,
        product_forward(weights_ref.at[1]),
        mask_ref,
        residual_ref,
        activation(read_middle, *norm_rows(table_ref, 1), act_two_ref, taps_ref, cols),
        lambda rows, part: part + (read_input(rows) + table_ref[13:14, :]),
        keep,
        cols,
    )
    table_ref[4:5, :], table_ref[5:6, :] = seen.finish(pixels)


def score_kernel(
    qkv_ref,
    proj_ref,
    residual_ref,
    table_ref,
    id_rows_ref,
    id_cols_ref,
    normed_ref,
    query_ref,
    key_ref,
    key_flip_ref,
    value_ref,
    soft_ref,
    out_flip_ref,
    output_ref,
    value_flip_ref,
    *scores_refs,
    score_scale,
):
    pixels, channels = residual_ref.shape
    own_pixels = output_ref.shape[0]
    wide = jnp.float32
    exponent = score_scale * 1.4426950408889634
    mean, inverse, gain, shift = norm_rows(table_ref, 2)
    scale = inverse * gain

    def normalise(start):
        rows = slice(start, start + KEY_ROWS)
        normed = (residual_ref[rows, :] - mean) * scale + shift
        normed_ref[rows, :] = normed.astype(jnp.bfloat16)

    def project(start):
        rows = slice(start, start + KEY_ROWS)
        normed = normed_ref[rows, :]
        query_ref[rows, :] = (
            jnp.dot(normed, qkv_ref[:, 0:channels], preferred_element_type=wide)
            + table_ref[14:15, :]
        ).astype(jnp.bfloat16)
        keys = jnp.dot(
            normed, qkv_ref[:, channels : 2 * channels], preferred_element_type=wide
        ).astype(jnp.bfloat16)
        key_ref[rows, :] = keys
        key_flip_ref[:, rows] = keys.T
        values = (
            jnp.dot(normed, qkv_ref[:, 2 * channels :], preferred_element_type=wide)
            + table_ref[15:16, :]
        ).astype(jnp.bfloat16)
        value_ref[rows, :] = values
        value_flip_ref[:, rows] = values.T

    normalise(0)
    for start in range(0, pixels, KEY_ROWS):
        if start + KEY_ROWS < pixels:
            normalise(start + KEY_ROWS)
        project(start)
    block = scores_refs[0].shape[1]
    steps = range(0, pixels, KEY_ROWS)

    def score(index):
        rows = slice(index * block, (index + 1) * block)
        for start in steps:
            keys = slice(start, start + KEY_ROWS)
            scores = lax.dot_general(
                key_ref[keys, :],
                query_ref[rows, :],
                (((1,), (1,)), ((), ())),
                preferred_element_type=wide,
            )
            same = widen(id_rows_ref[keys, :], block) == id_cols_ref[0:1, rows]
            scores_refs[index][keys, :] = jnp.where(same, scores, masked_score)

    def soften(index):
        rows = slice(index * block, (index + 1) * block)
        scores_ref = scores_refs[index]
        peak = jnp.full((8, block), masked_score, wide)
        for start in steps:
            scores = scores_ref[start : start + KEY_ROWS, :]
            peak = jnp.maximum(peak, jnp.max(scores.reshape(-1, 8, block), axis=0))
        peak = jnp.max(peak, axis=0, keepdims=True)
        total = jnp.zeros((8, block), wide)
        for start in steps:
            keys = slice(start, start + KEY_ROWS)
            powers = jnp.exp2((scores_ref[keys, :] - peak) * exponent)
            scores_ref[keys, :] = powers
            total = total + fold(powers)
        share = 1.0 / column_total(total)
        for start in steps:
            keys = slice(start, start + KEY_ROWS)
            soft_ref[keys, rows] = (scores_ref[keys, :] * share).astype(jnp.bfloat16)

    score(0)
    for index in range(len(scores_refs)):
        if index + 1 < len(scores_refs):
            score(index + 1)
        soften(index)
        rows = slice(index * block, (index + 1) * block)
        out_flip_ref[:, rows] = jnp.dot(
            value_flip_ref[...], soft_ref[:, rows], preferred_element_type=wide
        ).astype(jnp.bfloat16)
    height = lax.axis_index("height")
    own = pl.ds(pl.multiple_of(height * own_pixels, own_pixels), own_pixels)
    output_ref[...] = (
        residual_ref[own, :]
        + lax.dot_general(
            out_flip_ref[:, own],
            proj_ref[...],
            (((0,), (0,)), ((), ())),
            preferred_element_type=wide,
        )
        + table_ref[16:17, :]
    ).astype(jnp.bfloat16)


def own_quarter():
    height = lax.axis_index("height")
    return (height & 1) * 2 + ((height >> 1) & 1)


def attention_kernel(
    proj_ref,
    normed_ref,
    query_ref,
    key_flip_ref,
    value_ref,
    soft_ref,
    out_flip_ref,
    *refs,
    score_scale,
    count,
):
    pieces, (grad_ref, packed_ref, sums_ref), refs = (
        refs[:count],
        refs[count : count + 3],
        refs[count + 3 :],
    )
    pixels, channels = normed_ref.shape
    blocks = pixels // SCORE_ROWS
    grads_refs, refs = refs[-blocks:], refs[:-blocks]
    *mixed_refs, mixed_ref, back_ref, score_grad_ref, flip_ref = refs
    wide = jnp.float32
    height = lax.axis_index("height")
    own_pixels = pixels // count
    for place, piece in enumerate(pieces):
        start = pl.multiple_of((height ^ place) * own_pixels, own_pixels)
        last = piece.shape[0]
        grad_ref[pl.ds(start, own_pixels), :] = piece[last - own_pixels : last, :]
    quarter = channels // 4
    own = pl.ds(pl.multiple_of(own_quarter() * quarter, quarter), quarter)
    flip_ref[...] = normed_ref[:, own].T
    block, count = SCORE_ROWS, blocks
    steps = range(0, pixels, KEY_ROWS)

    def block_rows(index):
        return slice(index * block, (index + 1) * block)

    for start in range(0, pixels, 2 * block):
        rows = slice(start, start + 2 * block)
        back_ref[rows, :] = lax.dot_general(
            grad_ref[rows, :],
            proj_ref[...],
            (((1,), (1,)), ((), ())),
            preferred_element_type=wide,
        ).astype(jnp.bfloat16)

    def weigh(index):
        total = jnp.zeros((8, block), wide)
        for start in steps:
            keys = slice(start, start + KEY_ROWS)
            weight_grad = lax.dot_general(
                value_ref[keys, :],
                back_ref[block_rows(index), :],
                (((1,), (1,)), ((), ())),
                preferred_element_type=wide,
            )
            grads_refs[index][keys, :] = weight_grad
            total = total + fold(soft_ref[keys, block_rows(index)].astype(wide) * weight_grad)
        return column_total(total)

    def slope(index, dots):
        for start in steps:
            keys = slice(start, start + KEY_ROWS)
            weights = soft_ref[keys, block_rows(index)].astype(wide)
            score_grad_ref[keys, block_rows(index)] = (
                weights * (grads_refs[index][keys, :] - dots)
            ).astype(jnp.bfloat16)

    dots = weigh(0)
    for index in range(count):
        now, rows = dots, block_rows(index)
        if index + 1 < count:
            dots = weigh(index + 1)
        slope(index, now)
        packed_ref[rows, 2 * channels :] = jnp.dot(
            soft_ref[rows, :], back_ref[...], preferred_element_type=wide
        ).astype(jnp.bfloat16)
        query_grad = jnp.dot(
            key_flip_ref[...], score_grad_ref[:, rows], preferred_element_type=wide
        )
        packed_ref[rows, 0:channels] = (query_grad * score_scale).astype(jnp.bfloat16).T
    for start in range(0, pixels, 2 * block):
        rows = slice(start, start + 2 * block)
        packed_ref[rows, channels : 2 * channels] = (
            jnp.dot(score_grad_ref[rows, :], query_ref[...], preferred_element_type=wide)
            * score_scale
        ).astype(jnp.bfloat16)

    def pack(rows, carry):
        return (
            carry[0] + fold(packed_ref[rows, 0:channels].astype(wide)),
            carry[1] + fold(packed_ref[rows, 2 * channels :].astype(wide)),
            carry[2] + fold(grad_ref[rows, :].astype(wide)),
        )

    zeros = jnp.zeros((8, channels), wide)
    totals = zeros, zeros, zeros
    for start in range(0, pixels, CHUNK):
        totals = pack(pl.ds(start, CHUNK), totals)
    sums_ref[...] = jnp.zeros(sums_ref.shape, wide)
    for row, total in enumerate(totals):
        sums_ref[8 + row : 9 + row, :] = column_total(total)
    mixed_ref[:, 0 : 3 * channels] = jnp.dot(
        flip_ref[...], packed_ref[...], preferred_element_type=wide
    ).astype(jnp.bfloat16)
    mixed_ref[:, 3 * channels :] = jnp.dot(
        out_flip_ref[own, :], grad_ref[...], preferred_element_type=wide
    ).astype(jnp.bfloat16)
    share = quarter // len(mixed_refs)
    me = lax.axis_index("canvas")
    for step, target in enumerate(mixed_refs):
        target[...] = mixed_ref[pl.ds(pl.multiple_of((me ^ step) * share, share), share), :]


def third_kernel(
    qkv_ref,
    grad_ref,
    packed_ref,
    residual_ref,
    table_ref,
    act_two_ref,
    lanes_ref,
    old_sums_ref,
    total_ref,
    scales_ref,
    sums_ref,
    part_ref,
    flip_ref,
    columns_ref,
    *,
    cols,
):
    pixels, channels = residual_ref.shape
    block = 2 * FILL_ROWS
    wide = jnp.float32
    mean, inverse, gain, shift = norm_rows(table_ref, 2)
    zeros = jnp.zeros((8, channels), wide)

    sums = (zeros, zeros)
    for start in range(0, pixels, block):
        rows = pl.ds(start, block)
        normed_grad = lax.dot_general(
            packed_ref[rows, :], qkv_ref[...], (((1,), (1,)), ((), ())), preferred_element_type=wide
        )
        total_ref[rows, :] = normed_grad
        centered = residual_ref[rows, :] - mean
        sums = sums[0] + fold(normed_grad), sums[1] + fold(normed_grad * centered)
    sums = sums[0], sums[1] * inverse
    sums_ref[...] = old_sums_ref[...]
    sums_ref[5:6, :] = column_total(sums[1])
    sums_ref[6:7, :] = column_total(sums[0])
    norm_back(
        total_ref, False, sums, lambda rows: residual_ref[rows, :], table_ref, 2, pixels, scales_ref
    )
    narrow = narrow_back(total_ref, residual_ref, scales_ref)
    narrow = (grad_ref[:, own_lanes()].astype(wide) + narrow).astype(jnp.bfloat16)
    weight_part(act_two_ref, narrow, lanes_ref, flip_ref, columns_ref, part_ref, cols)


def second_kernel(
    old_total_ref,
    taps_ref,
    middle_ref,
    table_ref,
    act_one_ref,
    mask_ref,
    lanes_ref,
    weights_ref,
    old_sums_ref,
    part_two_ref,
    total_ref,
    scales_ref,
    sums_ref,
    keep_one_ref,
    send_one_ref,
    keep_two_ref,
    send_two_ref,
    flip_ref,
    columns_ref,
    part_ref,
    *,
    cols,
):
    pixels, channels = middle_ref.shape

    def read(rows):
        return middle_ref[rows, :]

    sums = finish_back(
        weights_ref.at[1],
        mask_ref,
        taps_ref,
        total_ref,
        read,
        table_ref,
        1,
        cols,
        old_total_ref,
        EARLY_ROWS,
    )
    norm_back(total_ref, True, sums, read, table_ref, 1, pixels, scales_ref)
    narrow = narrow_back(total_ref, middle_ref, scales_ref).astype(jnp.bfloat16)
    weight_part(act_one_ref, narrow, lanes_ref, flip_ref, columns_ref, part_ref, cols)
    sums_ref[...] = old_sums_ref[...]
    sums_ref[2:3, :] = column_total(sums[1])
    sums_ref[3:4, :] = column_total(sums[0])
    keep_half(part_ref, keep_one_ref, send_one_ref)
    keep_half(part_two_ref, keep_two_ref, send_two_ref)


def near_far():
    core = lax.axis_index("height") & 1
    return 1 + core, 2 - core


def keep_half(source_ref, keep_ref, send_ref):
    me = lax.axis_index("canvas")
    near, far = near_far()
    rows, width = keep_ref.shape[0] // 2, keep_ref.shape[1]
    for target_ref, flip in ((keep_ref, 0), (send_ref, near)):
        for slot, other in enumerate((0, far)):
            place = pl.ds(pl.multiple_of((me ^ flip ^ other) * width, width), width)
            target_ref[slot * rows : (slot + 1) * rows, :] = source_ref[:, place]


def first_kernel(
    total_two_ref,
    scales_ref,
    middle_ref,
    features_ref,
    table_ref,
    mask_ref,
    old_sums_ref,
    weights_ref,
    own_ref,
    sums_ref,
    partial_ref,
    total_ref,
    taps_ref,
    *,
    cols,
):
    def read(rows):
        return features_ref[rows, :].astype(jnp.float32)

    grad_sums = []

    def read_grad(rows):
        grad = scaled_back(total_two_ref, middle_ref, scales_ref, rows, rows)
        grad = grad.astype(jnp.bfloat16).astype(jnp.float32)
        grad_sums.append(fold(grad))
        return grad

    weights = weights_ref.at[0]
    begin_back(read_grad, weights, mask_ref, taps_ref, total_ref, total_ref.shape[0], cols)
    sums = finish_back(weights, mask_ref, taps_ref, total_ref, read, table_ref, 0, cols)
    partial_ref[0:8, :], partial_ref[8:16, :] = sums
    sums_ref[...] = old_sums_ref[...]
    sums_ref[0:1, :] = column_total(sums[1])
    sums_ref[1:2, :] = column_total(sums[0])
    sums_ref[4:5, :] = column_total(sum(grad_sums))
    count = own_ref.shape[0]
    own = pl.ds(pl.multiple_of(lax.axis_index("height") * count, count), count)
    own_ref[...] = total_ref[own, :]


def own_kernel(
    own_ref,
    partial_ref,
    features_ref,
    grad_ref,
    total_three_ref,
    residual_ref,
    scales_ref,
    table_ref,
    input_grad_ref,
):
    def read(rows):
        return features_ref[rows, :].astype(jnp.float32)

    sums = partial_ref[0:8, :], partial_ref[8:16, :]
    pixels = features_ref.shape[0]
    back = norm_back(own_ref, True, sums, read, table_ref, 0, pixels)
    count = own_ref.shape[0]
    own = pl.ds(pl.multiple_of(lax.axis_index("height") * count, count), count)
    total = scaled_back(total_three_ref, residual_ref, scales_ref, own, own)
    total = grad_ref[own, :].astype(jnp.float32) + total
    input_grad_ref[...] = (total + back(own, slice(0, count))).astype(jnp.bfloat16)


def place_kernel(*refs):
    joints, packed_ref = refs[:-1], refs[-1]
    share = packed_ref.shape[0] // len(joints)
    me = lax.axis_index("canvas")
    for step, joint in enumerate(joints):
        place = pl.ds(pl.multiple_of((me ^ step) * share, share), share)
        packed_ref[place, :] = joint[...]


def cut_kernel(packed_ref, *half_refs):
    rows = half_refs[0].shape[0]
    for index, half_ref in enumerate(half_refs):
        half_ref[...] = packed_ref[index * rows : (index + 1) * rows, :]


def spread_quarters(packed, flips, qkv_ref, proj_ref, qkv_hbm, proj_hbm, sems):
    quarter = packed[0].shape[0]
    inner = qkv_ref.shape[2]
    copies = []
    for index, packed_ref in enumerate(packed):
        owner = own_quarter() ^ flips[index]
        rows = pl.ds(pl.multiple_of(owner * quarter, quarter), quarter)
        qkv_ref[index] = packed_ref[:, 0:inner].astype(jnp.float32)
        proj_ref[index] = packed_ref[:, inner:].astype(jnp.float32)
        for which, (held, target) in enumerate(((qkv_ref, qkv_hbm), (proj_ref, proj_hbm))):
            copy = pltpu.make_async_copy(held.at[index], target.at[rows, :], sems.at[index, which])
            copy.start()
            copies.append(copy)
    return copies


def join_kernel(*refs):
    packed, (qkv_hbm, proj_hbm, qkv_ref, proj_ref, sems) = refs[:-5], refs[-5:]
    copies = spread_quarters(packed, [0, 2], qkv_ref, proj_ref, qkv_hbm, proj_hbm, sems)
    for copy in copies:
        copy.wait()


def halve_kernel(keep_ref, got_ref, hold_ref, send_ref):
    total = keep_ref[...].astype(jnp.float32) + got_ref[...].astype(jnp.float32)
    rows = hold_ref.shape[0]
    hold_ref[...] = total[0:rows]
    send_ref[0:rows, :] = total[rows:].astype(jnp.bfloat16)


def halve_both_kernel(
    keep_ref, got_ref, keep_two_ref, got_two_ref, hold_ref, send_ref, hold_two_ref
):
    rows = hold_ref.shape[0]
    halve_kernel(keep_ref, got_ref, hold_ref, send_ref)
    halve_kernel(keep_two_ref, got_two_ref, hold_two_ref, send_ref.at[rows : 2 * rows, :])


def last_kernel(
    chip_ref,
    both_a_ref,
    both_b_ref,
    old_qkv,
    old_proj,
    qkv_hbm,
    proj_hbm,
    qkv_ref,
    proj_ref,
    sems,
):
    copies = []
    rows = both_a_ref.shape[0]
    inner = qkv_ref.shape[2]
    chips = (chip_ref.at[0:rows, :], chip_ref.at[rows : 2 * rows, :])
    for index, piece_ref in enumerate((*chips, both_a_ref, both_b_ref)):
        start = ((own_quarter() ^ (1 if index < 2 else 3)) * 2 + index % 2) * rows
        target = pl.ds(pl.multiple_of(start, rows), rows)
        qkv_ref[index] = piece_ref[:, 0:inner].astype(jnp.float32)
        proj_ref[index] = piece_ref[:, inner:].astype(jnp.float32)
        for which, (held, whole) in enumerate(((qkv_ref, qkv_hbm), (proj_ref, proj_hbm))):
            copy = pltpu.make_async_copy(held.at[index], whole.at[target, :], sems.at[index, which])
            copy.start()
            copies.append(copy)
    for copy in copies:
        copy.wait()


def sums_kernel(
    sums_ref,
    got_sums_ref,
    hold_one_ref,
    hold_two_ref,
    got_ref,
    share_ref,
    gains_ref,
    shifts_ref,
    conv_ref,
    qv_ref,
    bias_ref,
):
    rows = hold_one_ref.shape[0]
    for which, hold_ref in enumerate((hold_one_ref, hold_two_ref)):
        got = got_ref[which * rows : (which + 1) * rows, :].astype(jnp.float32)
        share_ref[which] = (hold_ref[...] + got).reshape(share_ref.shape[1:])
    total = sums_ref[...] + got_sums_ref[...]
    for row, start in enumerate((0, 2, 5)):
        gains_ref[row : row + 1, :] = total[start : start + 1]
        shifts_ref[row : row + 1, :] = total[start + 1 : start + 2]
    conv_ref[0:1, :] = total[4:5]
    conv_ref[1:2, :] = total[7:8]
    qv_ref[...] = total[8:10]
    bias_ref[...] = total[10:11]


def call_kernel(kernel, outputs, scratch, operands, places, flops, limit, out_places=None, aliases={}):
    out_places = out_places or "v" * len(outputs)
    spaces = {
        "v": pl.BlockSpec(memory_space=pltpu.VMEM),
        "s": pl.BlockSpec(memory_space=pltpu.SMEM),
        "h": pl.BlockSpec(memory_space=pl.ANY),
        "o": pl.BlockSpec(memory_space=pltpu.VMEM),
        "a": pl.BlockSpec(memory_space=pl.ANY),
    }
    moved = 8 * flops // LANES
    held = {"v": pltpu.VMEM, "h": pltpu.HBM, "o": jax.ShapeDtypeStruct}
    operands = [
        pltpu.with_memory_space_constraint(array, pltpu.HBM) if place == "h" else array
        for array, place in zip(operands, places)
    ]
    return pl.pallas_call(
        kernel,
        out_shape=[held[place](*output) for output, place in zip(outputs, out_places)],
        in_specs=[spaces[place] for place in places],
        out_specs=[spaces[place] for place in out_places],
        scratch_shapes=scratch,
        input_output_aliases=aliases,
        compiler_params=pltpu.CompilerParams(vmem_limit_bytes=limit * 2**20),
        cost_estimate=pl.CostEstimate(flops=flops, bytes_accessed=moved, transcendentals=0),
    )(*operands)


def send_height(block, step):
    size = lax.axis_size("height")
    return lax.ppermute(block, "height", [(i, i ^ step) for i in range(size)])


def with_cores(blocks, other):
    pieces = [blocks[0], other]
    for block in blocks[1:]:
        pieces += [block, send_height(block, 1)]
    return pieces


def send_canvas(block, step):
    size = lax.axis_size("canvas")
    return lax.ppermute(block, "canvas", [(i, i ^ step) for i in range(size)])


def send_phase(block, phase):
    canvases, size = lax.axis_size("canvas"), lax.axis_size("height")
    pairs = []
    for canvas in range(canvases):
        for height in range(size):
            step = 2 if (height ^ phase) & 1 else 1
            pairs.append((canvas * size + height, (canvas ^ step) * size + height))
    return lax.ppermute(block, ("canvas", "height"), pairs)


def trade_canvas(pieces):
    return [pieces[0]] + [send_canvas(piece, step) for step, piece in enumerate(pieces) if step]


def whole_canvas(
    features,
    tile_ids,
    norm_gains,
    norm_shifts,
    conv_weights,
    conv_biases,
    qkv_weight,
    qv_bias,
    proj_weight,
    proj_bias,
    cotangent,
):
    height_size = lax.axis_size("height")
    canvas_size = lax.axis_size("canvas")
    local_rows, cols, channels = features.shape[1:]
    all_rows = tile_ids.shape[1]
    pixels = all_rows * cols
    own_pixels = local_rows * cols
    out_share = channels // height_size
    ci_share = channels // canvas_size
    quarter = channels // 4
    row_share = quarter // canvas_size
    low, wide = jnp.bfloat16, jnp.float32

    own_features = features.reshape(own_pixels, channels)
    own_grad = cotangent.reshape(own_pixels, channels)
    steps = range(2, height_size, 2)
    held_features = [own_features] + [send_height(own_features, step) for step in steps]
    plane = ((pixels, channels), low)
    plane_wide = ((pixels, channels), wide)
    sums_shape = ((16, channels), wide)
    mixed_shapes = [((row_share, 4 * channels), low)] * canvas_size
    taps = pltpu.VMEM((pixels + 2 * cols, 3 * channels), low)
    held_wide = pltpu.VMEM((pixels, channels), wide)
    flipped = pltpu.VMEM((channels, pixels), low)
    narrow = pltpu.VMEM((NARROW, pixels), low)
    columns = pltpu.VMEM((9 * out_share, pixels), low)
    part_held = pltpu.VMEM((9 * out_share, channels), low)
    sem = pltpu.SemaphoreType.DMA
    conv_flops = 2 * 9 * pixels * channels * channels
    dot_flops = 2 * pixels * channels * channels
    score_flops = 2 * pixels * pixels * channels
    scale = channels ** (-0.5)

    (
        held_conv,
        turned,
        held_qkv,
        held_proj,
        params,
        mask,
        lane_mask,
        id_rows,
        id_cols,
    ) = call_kernel(
        functools.partial(hold_kernel, cols=cols),
        [
            (conv_weights.shape, low),
            ((2, 3, channels, 3 * channels), low),
            (qkv_weight.shape, low),
            (proj_weight.shape, low),
            ((24, channels), wide),
            ((2, pixels, LANES), wide),
            ((8, pixels), wide),
            ((pixels, LANES), jnp.int32),
            ((8, pixels), jnp.int32),
        ],
        [
            pltpu.SMEM(tile_ids.shape, jnp.int32),
            pltpu.VMEM(norm_gains.shape, wide),
            pltpu.VMEM(norm_shifts.shape, wide),
            pltpu.VMEM(conv_biases.shape, wide),
            pltpu.VMEM(qv_bias.shape, wide),
            pltpu.VMEM((1, channels), wide),
            sem((27,)),
        ],
        [
            tile_ids,
            norm_gains,
            norm_shifts,
            conv_biases,
            conv_weights,
            qkv_weight,
            proj_weight,
            qv_bias,
            proj_bias.reshape(1, channels),
        ],
        "h" * 9,
        conv_flops,
        8,
    )
    held_features[1:] = [
        lax.optimization_barrier((params, block))[1] for block in held_features[1:]
    ]
    other_core = send_height(jnp.concatenate([own_features, own_grad], axis=0), 1)
    pieces = with_cores(held_features, other_core)
    far_grad, *pieces[4::2] = lax.optimization_barrier((own_grad, *held_features[2:]))
    held_grads = [own_grad, send_height(own_grad, 2)]
    held_grads[1], pieces[2] = lax.optimization_barrier((held_grads[1], held_features[1]))
    held_grads += [send_height(far_grad, step) for step in steps[1:]]

    all_features, act_one, middle, act_two, residual, table = call_kernel(
        functools.partial(conv_kernel, cols=cols, count=height_size),
        [plane, plane, plane_wide, plane, plane_wide, ((24, channels), wide)],
        [pltpu.VMEM((own_pixels, channels), low), taps, sem],
        [*pieces, held_conv, params, mask],
        "h" + "v" * (height_size + 2),
        2 * conv_flops,
        16,
    )
    residual, *held_grads = lax.optimization_barrier((residual, *held_grads))
    grad_pieces = with_cores(held_grads, other_core)
    normed, query, key, key_flip, value, soft, out_flip, output = call_kernel(
        functools.partial(score_kernel, score_scale=scale),
        [
            plane,
            plane,
            plane,
            ((channels, pixels), low),
            plane,
            ((pixels, pixels), low),
            ((channels, pixels), low),
            ((own_pixels, channels), low),
        ],
        [
            flipped,
            *[pltpu.VMEM((pixels, SCORE_ROWS), wide)] * (pixels // SCORE_ROWS),
        ],
        [
            held_qkv,
            held_proj,
            residual,
            table,
            id_rows,
            id_cols,
        ],
        "vvvvvv",
        3 * dot_flops + 2 * score_flops,
        20,
        "v" * 7 + "o",
    )
    normed, *grad_pieces = lax.optimization_barrier((normed, *grad_pieces))
    all_grad, packed, sums, *mixed = call_kernel(
        functools.partial(attention_kernel, score_scale=scale, count=height_size),
        [plane, ((pixels, 3 * channels), low), sums_shape, *mixed_shapes],
        [
            pltpu.VMEM((quarter, 4 * channels), low),
            pltpu.VMEM((pixels, channels), low),
            pltpu.VMEM((pixels, pixels), low),
            pltpu.VMEM((quarter, pixels), low),
            *[pltpu.VMEM((pixels, SCORE_ROWS), wide)] * (pixels // SCORE_ROWS),
        ],
        [held_proj, normed, query, key_flip, value, soft, out_flip, *grad_pieces],
        "v" * (7 + height_size),
        3 * dot_flops + 4 * score_flops,
        20,
    )
    mixed = trade_canvas(mixed)
    total_three, scales_three, sums, part_two = call_kernel(
        functools.partial(third_kernel, cols=cols),
        [plane_wide, ((8, channels), wide), sums_shape, ((9 * out_share, channels), low)],
        [narrow, columns],
        [held_qkv, all_grad, packed, residual, table, act_two, lane_mask, sums],
        "vvvvvvvv",
        3 * dot_flops + conv_flops // height_size,
        16,
    )
    half_total, half_taps, sums = call_kernel(
        functools.partial(turn_kernel, cols=cols),
        [plane_wide, (taps.shape, low), sums_shape],
        [],
        [all_grad, total_three, scales_three, residual, mask, turned, sums],
        "vvvvvvv",
        conv_flops // 2,
        16,
    )
    half_total, *mixed = lax.optimization_barrier((half_total, *mixed))
    mixed_sum = mixed[0].astype(wide)
    for piece in mixed[1:]:
        mixed_sum = mixed_sum + piece.astype(wide)
    mixed_sum = mixed_sum.astype(low)
    joints = trade_canvas([mixed_sum] * canvas_size)
    halves = [((2 * 9 * out_share, ci_share), low)] * 4
    total_two, scales, sums, keep_one, send_one, keep_two, send_two = call_kernel(
        functools.partial(second_kernel, cols=cols),
        [plane_wide, ((8, channels), wide), sums_shape, *halves],
        [narrow, columns, part_held],
        [half_total, half_taps, middle, table, act_one, mask, lane_mask, turned, sums, part_two],
        "v" * 10,
        conv_flops // 2,
        20,
    )
    total_two, *joints = lax.optimization_barrier((total_two, *joints))
    (own_mixed,) = call_kernel(
        place_kernel,
        [((quarter, 4 * channels), low)],
        [],
        joints,
        "v" * canvas_size,
        1,
        12,
    )
    own_mixed, send_one, send_two = lax.optimization_barrier((own_mixed, send_one, send_two))
    chip_mixed = send_height(own_mixed, 2)
    core_mixed = send_height(own_mixed, 1)
    got_one, got_two = send_phase(send_one, 0), send_phase(send_two, 0)
    own_total, sums, partial_sums = call_kernel(
        functools.partial(first_kernel, cols=cols),
        [((own_pixels, channels), wide), sums_shape, sums_shape],
        [held_wide, taps],
        [total_two, scales, middle, all_features, table, mask, sums, turned],
        "vvvvvvvv",
        1,
        20,
    )
    got_sums, own_sums = send_phase(sums, 0), sums
    sums, core_mixed, got_one, got_two = lax.optimization_barrier(
        (sums, core_mixed, got_one, got_two)
    )
    share_rows = 9 * out_share
    hold_one, send_share, hold_two = call_kernel(
        halve_both_kernel,
        [
            ((share_rows, ci_share), wide),
            ((2 * share_rows, ci_share), low),
            ((share_rows, ci_share), wide),
        ],
        [],
        [keep_one, got_one, keep_two, got_two],
        "vvvv",
        1,
        12,
    )
    got_share = send_phase(send_share, 1)

    def widened(count, rows):
        return [
            pltpu.VMEM((count, rows, 3 * channels), wide),
            pltpu.VMEM((count, rows, channels), wide),
            sem((count, 2)),
        ]

    grad_shapes = [(qkv_weight.shape, wide), (proj_weight.shape, wide)]
    core_mixed, hold_one = lax.optimization_barrier((core_mixed, hold_one))
    qkv_grad, proj_grad = call_kernel(
        join_kernel,
        grad_shapes,
        widened(2, quarter),
        [own_mixed, core_mixed],
        "vv",
        1,
        12,
        "hh",
    )
    qkv_grad, chip_mixed, got_sums = lax.optimization_barrier((qkv_grad, chip_mixed, got_sums))
    sums = own_sums + got_sums
    got_sums = send_phase(sums, 1)
    chip_halves = call_kernel(
        cut_kernel,
        [((quarter // 2, 4 * channels), low)] * 2,
        [],
        [chip_mixed],
        "v",
        1,
        12,
    )
    both_halves = [send_height(half, 1) for half in chip_halves]
    qkv_grad, proj_grad = call_kernel(
        last_kernel,
        grad_shapes,
        widened(4, quarter // 2),
        [chip_mixed, *both_halves, qkv_grad, proj_grad],
        "vvvhh",
        1,
        12,
        "hh",
        {3: 0, 4: 1},
    )
    qkv_grad, own_total = lax.optimization_barrier((qkv_grad, own_total))
    (input_grad,) = call_kernel(
        own_kernel,
        [((own_pixels, channels), low)],
        [],
        [
            own_total,
            partial_sums,
            all_features,
            all_grad,
            total_three,
            residual,
            scales_three,
            table,
        ],
        "v" * 8,
        dot_flops // 4,
        12,
        "o",
    )
    input_grad, got_share, got_sums = lax.optimization_barrier((input_grad, got_share, got_sums))
    vector_shapes = [norm_gains.shape, norm_shifts.shape, conv_biases.shape, qv_bias.shape]
    conv_grad, gains_grad, shifts_grad, biases_grad, qv_grad, proj_bias_grad = call_kernel(
        sums_kernel,
        [((2, 3, 3, out_share, ci_share), wide)]
        + [(shape, wide) for shape in vector_shapes + [(1, channels)]],
        [],
        [sums, got_sums, hold_one, hold_two, got_share],
        "vvvvv",
        1,
        12,
        "o" * 6,
    )
    own_shape = (1, local_rows, cols, channels)
    return (
        output.reshape(own_shape),
        input_grad.reshape(own_shape),
        gains_grad,
        shifts_grad,
        jnp.swapaxes(conv_grad, 3, 4),
        biases_grad,
        qkv_grad,
        qv_grad,
        proj_grad,
        proj_bias_grad.reshape(channels),
    )


def on_device(*arrays):
    features, tile_ids = arrays[0], arrays[1]
    local_rows, cols, channels = features.shape[1:]
    pixels = tile_ids.shape[1] * cols
    height_size, canvas_size = lax.axis_size("height"), lax.axis_size("canvas")
    powers = all(size & (size - 1) == 0 for size in (height_size, canvas_size, cols))
    fits = (
        powers
        and height_size > 2
        and canvas_size == 4
        and channels == LANES * canvas_size
        and pixels <= MOST_PIXELS
        and pixels % FILL_ROWS == 0
        and pixels >= EARLY_ROWS
        and FILL_ROWS % CHUNK == 0
        and pixels % SCORE_ROWS == 0
        and pixels % KEY_ROWS == 0
        and (local_rows * cols) % LANES == 0
        and CHUNK % cols == 0
        and cols % 16 == 0
        and channels % (LANES * canvas_size) == 0
        and 2 * channels == NARROW * height_size
    )
    return whole_canvas(*arrays) if fits else split_canvas(*arrays)


def solution(mesh):
    in_specs = (
        P("canvas", "height", None, None),
        P("canvas", None),
        P(),
        P(),
        P(),
        P(),
        P(),
        P(),
        P(),
        P(),
        P("canvas", "height", None, None),
    )
    out_specs = (
        P("canvas", "height", None, None),
        P("canvas", "height", None, None),
        P(),
        P(),
        P(None, None, None, "canvas", "height"),
        P(),
        P(),
        P(),
        P(),
        P(),
    )
    return jax.shard_map(
        on_device, mesh=mesh, in_specs=in_specs, out_specs=out_specs, check_vma=False
    )
```

```python
import functools

import jax
import jax.numpy as jnp
from jax import lax
from jax.experimental import pallas as pl
from jax.experimental.pallas import tpu as pltpu
from jax.sharding import PartitionSpec as P

GROUPS = 32


epsilon = 1e-06
masked_score = -1e30
MOST_PIXELS = 1024
LANES = 128
NARROW = 128
CHUNK = 128
FILL_ROWS = 256
EARLY_ROWS = 512
SCORE_ROWS = 256
KEY_ROWS = 256


def extended(block, sides, width):
    for axis, dim in sides:
        count = lax.axis_size(axis)
        forward = [(i, i + 1) for i in range(count - 1)]
        backward = [(target, source) for source, target in forward]
        low = lax.ppermute(
            lax.slice_in_dim(block, block.shape[dim] - width, None, axis=dim), axis, forward
        )
        high = lax.ppermute(lax.slice_in_dim(block, 0, width, axis=dim), axis, backward)
        block = jnp.concatenate([low, block, high], axis=dim)
    return block


def group_total(vector):
    return vector.reshape(GROUPS, -1).sum(axis=1)


def spread_groups(vector, channels):
    return jnp.repeat(vector, channels // GROUPS)


def norm_forward(values, gain, shift, members):
    channels = values.shape[1]
    totals = lax.psum(group_total(jnp.sum(values, axis=0)), "height")
    centered = values - spread_groups(totals / members, channels)
    squares = lax.psum(group_total(jnp.sum(centered * centered, axis=0)), "height")
    inverse = spread_groups(lax.rsqrt(squares / members + epsilon), channels)
    normed = centered * inverse
    return (normed, inverse, normed * gain + shift)


def norm_backward(grad_in, normed, inverse, gain, members):
    channels = grad_in.shape[1]
    scaled = grad_in * gain
    both_sums = lax.psum(
        (group_total(jnp.sum(scaled, axis=0)), group_total(jnp.sum(scaled * normed, axis=0))),
        "height",
    )
    mean_grad = spread_groups(both_sums[0] / members, channels)
    mean_cross = spread_groups(both_sums[1] / members, channels)
    result = inverse * (scaled - mean_grad - normed * mean_cross)
    return (result, jnp.sum(grad_in * normed, axis=0), jnp.sum(grad_in, axis=0))


def swish(values):
    return values * jax.nn.sigmoid(values)


def swish_slope(values):
    sigmoid_part = jax.nn.sigmoid(values)
    return sigmoid_part * (1.0 + values * (1.0 - sigmoid_part))


def tap_columns(padded, row_mask, local_rows, canvas_cols):
    pieces = []
    for row_tap in range(3):
        rows_taken = padded[row_tap : row_tap + local_rows] * row_mask[:, row_tap, None, None]
        for col_tap in range(3):
            pieces.append(rows_taken[:, col_tap : col_tap + canvas_cols])
    stacked = jnp.concatenate(pieces, axis=2)
    return stacked.reshape(local_rows * canvas_cols, stacked.shape[2])


def conv_forward(acts, row_mask, weight, bias):
    local_rows, canvas_cols, channels = acts.shape
    rimmed = extended(acts, (("height", 0),), 1)
    padded = jnp.pad(rimmed, ((0, 0), (1, 1), (0, 0)))
    gathered = tap_columns(padded, row_mask, local_rows, canvas_cols)
    result = (
        jnp.dot(
            gathered, weight.reshape(9 * channels, channels), preferred_element_type=jnp.float32
        )
        + bias
    )
    return (result, gathered)


def conv_backward(grad_low, row_mask, weight, gathered):
    local_rows, canvas_cols, channels = grad_low.shape
    flat_grad = grad_low.reshape(local_rows * canvas_cols, channels)
    weight_grad = lax.dot_general(
        gathered, flat_grad, (((0,), (0,)), ((), ())), preferred_element_type=jnp.float32
    )
    rimmed = extended(grad_low, (("height", 0),), 1)
    padded = jnp.pad(rimmed, ((0, 0), (1, 1), (0, 0)))
    grad_taps = tap_columns(padded, row_mask, local_rows, canvas_cols)
    flipped = jnp.transpose(weight[::-1, ::-1], (0, 1, 3, 2)).reshape(9 * channels, channels)
    input_part = jnp.dot(grad_taps, flipped, preferred_element_type=jnp.float32)
    return (
        input_part,
        weight_grad.reshape(3, 3, channels, channels),
        jnp.sum(flat_grad.astype(jnp.float32), axis=0),
    )


def take_rows(array, offset, count):
    return lax.dynamic_slice_in_dim(array, offset, count)


def score_grads(
    queries, out_grad, log_total, row_dots, query_ids, key_rows, value_rows, key_ids, score_scale
):
    scores = (
        lax.dot_general(
            queries, key_rows, (((1,), (1,)), ((), ())), preferred_element_type=jnp.float32
        )
        * score_scale
    )
    same_tile = query_ids[:, None] == key_ids[None, :]
    softmax_block = jnp.exp(jnp.where(same_tile, scores - log_total[:, None], masked_score))
    weight_grad = lax.dot_general(
        out_grad, value_rows, (((1,), (1,)), ((), ())), preferred_element_type=jnp.float32
    )
    score_grad = (softmax_block * (weight_grad - row_dots[:, None])).astype(jnp.bfloat16)
    return (softmax_block.astype(jnp.bfloat16), score_grad)


def split_canvas(
    features,
    tile_ids,
    norm_gains,
    norm_shifts,
    conv_weights,
    conv_biases,
    qkv_weight,
    qv_bias,
    proj_weight,
    proj_bias,
    cotangent,
):
    height_size = lax.axis_size("height")
    local_rows = features.shape[1]
    canvas_cols = features.shape[2]
    channels = features.shape[3]
    pixels = local_rows * canvas_cols
    row_ids = tile_ids[0]
    all_rows = row_ids.shape[0]
    members = float(all_rows * canvas_cols * (channels // GROUPS))
    score_scale = channels ** (-0.5)
    first_row = lax.axis_index("height") * local_rows
    edge_ids = jnp.full((1,), -1, jnp.int32)
    padded_ids = jnp.concatenate([edge_ids, row_ids, edge_ids])
    near_ids = lax.dynamic_slice_in_dim(padded_ids, first_row, local_rows + 2)
    own_rows = near_ids[1 : local_rows + 1]
    row_mask = jnp.stack(
        [near_ids[row_tap : row_tap + local_rows] == own_rows for row_tap in range(3)], axis=1
    ).astype(jnp.bfloat16)
    key_ids = jnp.repeat(row_ids, canvas_cols)
    query_ids = jnp.repeat(own_rows, canvas_cols)
    grid_shape = (local_rows, canvas_cols, channels)
    inputs = features[0].reshape(pixels, channels).astype(jnp.float32)
    normed_one, inverse_one, pre_one = norm_forward(inputs, norm_gains[0], norm_shifts[0], members)
    act_one = swish(pre_one).astype(jnp.bfloat16).reshape(grid_shape)
    middle, taps_one = conv_forward(act_one, row_mask, conv_weights[0], conv_biases[0])
    normed_two, inverse_two, pre_two = norm_forward(middle, norm_gains[1], norm_shifts[1], members)
    act_two = swish(pre_two).astype(jnp.bfloat16).reshape(grid_shape)
    branch, taps_two = conv_forward(act_two, row_mask, conv_weights[1], conv_biases[1])
    residual = inputs + branch
    normed_three, inverse_three, pre_three = norm_forward(
        residual, norm_gains[2], norm_shifts[2], members
    )
    attn_input = pre_three.astype(jnp.bfloat16)
    mixed = jnp.dot(attn_input, qkv_weight, preferred_element_type=jnp.float32)
    queries = (mixed[:, :channels] + qv_bias[0]).astype(jnp.bfloat16)
    key_rows = mixed[:, channels : 2 * channels].astype(jnp.bfloat16)
    value_rows = (mixed[:, 2 * channels :] + qv_bias[1]).astype(jnp.bfloat16)
    running_max = jnp.full((pixels,), masked_score, jnp.float32)
    key_piece = lax.all_gather(key_rows, "height", axis=0, tiled=True)
    value_piece = lax.all_gather(value_rows, "height", axis=0, tiled=True)
    scores = (
        lax.dot_general(
            queries, key_piece, (((1,), (1,)), ((), ())), preferred_element_type=jnp.float32
        )
        * score_scale
    )
    same_tile = query_ids[:, None] == key_ids[None, :]
    scores = jnp.where(same_tile, scores, masked_score)
    new_max = jnp.maximum(running_max, jnp.max(scores, axis=1))
    weights = jnp.where(same_tile, jnp.exp(scores - new_max[:, None]), 0.0)
    summed_out = jnp.dot(
        weights.astype(jnp.bfloat16), value_piece, preferred_element_type=jnp.float32
    )
    total_weight = jnp.sum(weights, axis=1)
    log_total = new_max + jnp.log(total_weight)
    attended = summed_out / total_weight[:, None]
    attended_low = attended.astype(jnp.bfloat16)
    output = (
        residual
        + jnp.dot(attended_low, proj_weight, preferred_element_type=jnp.float32)
        + proj_bias
    )
    out_grad = cotangent[0].reshape(pixels, channels)
    out_grad_full = out_grad.astype(jnp.float32)
    proj_grad = lax.dot_general(
        attended_low, out_grad, (((0,), (0,)), ((), ())), preferred_element_type=jnp.float32
    )
    proj_bias_grad = jnp.sum(out_grad_full, axis=0)
    attended_grad = lax.dot_general(
        out_grad, proj_weight, (((1,), (1,)), ((), ())), preferred_element_type=jnp.float32
    ).astype(jnp.bfloat16)
    row_dots = jnp.sum(attended_grad.astype(jnp.float32) * attended, axis=1)
    block_rows = pixels * min(height_size, 8)
    zero_block = jnp.zeros((pixels, channels), jnp.float32)
    key_all, value_all = (
        lax.all_gather(key_rows, "height", axis=0, tiled=True),
        lax.all_gather(value_rows, "height", axis=0, tiled=True),
    )
    query_all, grad_all = (
        lax.all_gather(queries, "height", axis=0, tiled=True),
        lax.all_gather(attended_grad, "height", axis=0, tiled=True),
    )
    total_all, dots_all = (
        lax.all_gather(log_total, "height", axis=0, tiled=True),
        lax.all_gather(row_dots, "height", axis=0, tiled=True),
    )

    def own_query_step(running, block_index):
        offset = block_index * block_rows
        key_part = take_rows(key_all, offset, block_rows)
        rounded, score_grad = score_grads(
            queries,
            attended_grad,
            log_total,
            row_dots,
            query_ids,
            key_part,
            take_rows(value_all, offset, block_rows),
            take_rows(key_ids, offset, block_rows),
            score_scale,
        )
        return (
            running
            + jnp.dot(score_grad, key_part, preferred_element_type=jnp.float32) * score_scale,
            None,
        )

    def own_key_step(running, block_index):
        offset = block_index * block_rows
        query_part = take_rows(query_all, offset, block_rows)
        grad_part = take_rows(grad_all, offset, block_rows)
        rounded, score_grad = score_grads(
            query_part,
            grad_part,
            take_rows(total_all, offset, block_rows),
            take_rows(dots_all, offset, block_rows),
            take_rows(key_ids, offset, block_rows),
            key_rows,
            value_rows,
            query_ids,
            score_scale,
        )
        key_part = (
            lax.dot_general(
                score_grad, query_part, (((0,), (0,)), ((), ())), preferred_element_type=jnp.float32
            )
            * score_scale
        )
        value_part = lax.dot_general(
            rounded, grad_part, (((0,), (0,)), ((), ())), preferred_element_type=jnp.float32
        )
        return ((running[0] + key_part, running[1] + value_part), None)

    block_count = key_all.shape[0] // block_rows
    query_grad, unused_one = lax.scan(own_query_step, zero_block, jnp.arange(block_count))
    (key_grad, value_grad), unused_two = lax.scan(
        own_key_step, (zero_block, zero_block), jnp.arange(block_count)
    )
    query_low = query_grad.astype(jnp.bfloat16)
    key_low = key_grad.astype(jnp.bfloat16)
    value_low = value_grad.astype(jnp.bfloat16)
    stacked_grad = jnp.concatenate([query_low, key_low, value_low], axis=1)
    qkv_grad = lax.dot_general(
        attn_input, stacked_grad, (((0,), (0,)), ((), ())), preferred_element_type=jnp.float32
    )
    qv_grad = jnp.stack(
        [
            jnp.sum(query_low.astype(jnp.float32), axis=0),
            jnp.sum(value_low.astype(jnp.float32), axis=0),
        ]
    )
    normed_grad = lax.dot_general(
        stacked_grad, qkv_weight, (((1,), (1,)), ((), ())), preferred_element_type=jnp.float32
    )
    back_three, gain_three, shift_three = norm_backward(
        normed_grad, normed_three, inverse_three, norm_gains[2], members
    )
    residual_grad = out_grad_full + back_three
    grad_two = residual_grad.astype(jnp.bfloat16).reshape(grid_shape)
    act_two_grad, weight_two_grad, bias_two_grad = conv_backward(
        grad_two, row_mask, conv_weights[1], taps_two
    )
    middle_grad, gain_two, shift_two = norm_backward(
        act_two_grad * swish_slope(pre_two), normed_two, inverse_two, norm_gains[1], members
    )
    grad_one = middle_grad.astype(jnp.bfloat16).reshape(grid_shape)
    act_one_grad, weight_one_grad, bias_one_grad = conv_backward(
        grad_one, row_mask, conv_weights[0], taps_one
    )
    input_back, gain_one, shift_one = norm_backward(
        act_one_grad * swish_slope(pre_one), normed_one, inverse_one, norm_gains[0], members
    )
    input_grad = residual_grad + input_back
    conv_grad = jnp.stack([weight_one_grad, weight_two_grad])
    conv_part = lax.psum_scatter(conv_grad, "height", scatter_dimension=4, tiled=True)
    conv_part = lax.psum_scatter(
        conv_part.astype(jnp.bfloat16), "canvas", scatter_dimension=3, tiled=True
    ).astype(jnp.float32)
    summed = lax.psum(
        (
            jnp.stack([gain_one, gain_two, gain_three]),
            jnp.stack([shift_one, shift_two, shift_three]),
            jnp.stack([bias_one_grad, bias_two_grad]),
            qkv_grad,
            qv_grad,
            proj_grad,
            proj_bias_grad,
        ),
        ("canvas", "height"),
    )
    return (
        output.astype(jnp.bfloat16).reshape((1,) + grid_shape),
        input_grad.astype(jnp.bfloat16).reshape((1,) + grid_shape),
        summed[0],
        summed[1],
        conv_part,
        summed[2],
        summed[3],
        summed[4],
        summed[5],
        summed[6],
    )


def fold(block):
    rows, width = block.shape
    return jnp.sum(block.reshape(rows // 8, 8, width), axis=0)


def group_lanes(block, group):
    lane = lax.broadcasted_iota(jnp.int32, block.shape, 1)
    width = block.shape[1]
    step = 1
    while step < group:
        above = pltpu.roll(block, step, 1)
        below = pltpu.roll(block, width - step, 1)
        block = block + jnp.where((lane & step) != 0, above, below)
        step *= 2
    return block


def group_mean(partial, members):
    spread = group_lanes(partial, partial.shape[1] // GROUPS)
    return jnp.sum(spread, axis=0, keepdims=True) * (1.0 / members)


def widen(block, width):
    return jnp.concatenate([block] * (width // block.shape[1]), axis=1)


def each_block(pixels, block, body, carry=0):
    def step(index, carry):
        return body(pl.ds(pl.multiple_of(index * block, block), block), carry)

    return lax.fori_loop(0, pixels // block, step, carry)


def each_chunk(pixels, body, carry):
    return each_block(pixels, CHUNK, body, carry)


def aligned(start, step):
    return start if isinstance(start, int) else pl.multiple_of(start, step)


class RunningStats:
    def __init__(self, channels):
        self.width = channels // GROUPS
        self.reference = None
        self.sums = self.squares = jnp.zeros((8, channels), jnp.float32)

    def add(self, block):
        if self.reference is None:
            self.reference = group_mean(block[0:8], 8.0 * self.width)
        offset = block - self.reference
        self.sums = self.sums + fold(offset)
        self.squares = self.squares + fold(offset * offset)

    def finish(self, pixels):
        both = group_lanes(jnp.concatenate([self.sums, self.squares], axis=0), self.width)
        share = 1.0 / (pixels * self.width)
        offset = column_total(both[0:8]) * share
        variance = column_total(both[8:16]) * share - offset * offset
        return self.reference + offset, lax.rsqrt(jnp.maximum(variance, 0.0) + epsilon)


def put_taps(taps_ref, block, rows, cols):
    count, channels = block.shape
    place = lax.broadcasted_iota(jnp.int32, block.shape, 0) & (cols - 1)
    left = jnp.where(place == 0, 0.0, pltpu.roll(block, 1, 0))
    right = jnp.where(place == cols - 1, 0.0, pltpu.roll(block, count - 1, 0))
    inner = pl.ds(aligned(rows.start + cols, cols), count)
    taps_ref[inner, 0:channels] = left.astype(jnp.bfloat16)
    taps_ref[inner, channels : 2 * channels] = block.astype(jnp.bfloat16)
    taps_ref[inner, 2 * channels :] = right.astype(jnp.bfloat16)


def clear_edges(taps_ref, cols):
    edge = jnp.zeros((cols, taps_ref.shape[1]), taps_ref.dtype)
    taps_ref[0:cols, :] = edge
    taps_ref[taps_ref.shape[0] - cols :, :] = edge


def begin_conv(taps_ref, product, total_ref, fill, first, cols):
    for start in range(0, total_ref.shape[0], FILL_ROWS):
        for inner in range(start, start + FILL_ROWS, CHUNK):
            fill(pl.ds(inner, CHUNK))
        rows = pl.ds(start, FILL_ROWS)
        total_ref[rows, :] = first(rows, product(taps_ref, pl.ds(start + cols, FILL_ROWS), 1))


def add_rows(taps_ref, product, mask_ref, total_ref, stop, cols):
    rows = pl.ds(0, stop)
    part = product(taps_ref, rows, 0)
    total_ref[rows, :] += widen(mask_ref[0, rows, :], total_ref.shape[1]) * part


def end_conv(taps_ref, product, mask_ref, total_ref, last, cols, old_ref=None, pending=None):
    pixels, channels = total_ref.shape
    old_ref = total_ref if old_ref is None else old_ref
    pending = pixels if pending is None else pending
    for start in range(0, pixels, FILL_ROWS):
        rows = pl.ds(start, FILL_ROWS)
        value = old_ref[rows, :]
        for row_tap in (0, 2) if start >= pending else (2,):
            part = product(taps_ref, pl.ds(start + row_tap * cols, FILL_ROWS), row_tap)
            value = value + widen(mask_ref[row_tap // 2, rows, :], channels) * part
        total_ref[rows, :] = last(rows, value)


def run_conv(taps_ref, product, mask_ref, total_ref, fill, first, last, cols):
    begin_conv(taps_ref, product, total_ref, fill, first, cols)
    add_rows(taps_ref, product, mask_ref, total_ref, total_ref.shape[0], cols)
    end_conv(taps_ref, product, mask_ref, total_ref, last, cols)


def product_forward(weight_ref):
    channels = weight_ref.shape[-1]

    def product(taps_ref, shifted, row_tap):
        return jnp.dot(
            taps_ref[shifted, :],
            weight_ref[row_tap].reshape(3 * channels, channels),
            preferred_element_type=jnp.float32,
        )

    return product


def product_backward(weight_ref):
    def product(taps_ref, shifted, row_tap):
        return lax.dot_general(
            taps_ref[shifted, :],
            weight_ref[row_tap],
            (((1,), (1,)), ((), ())),
            preferred_element_type=jnp.float32,
        )

    return product


def activation(read, mean, inverse, gain, shift, act_ref, taps_ref, cols):
    scale, offset = 0.5 * inverse * gain, 0.5 * shift

    def fill(rows):
        half = (read(rows) - mean) * scale + offset
        act = half * (1.0 + jnp.tanh(half))
        act_ref[rows, :] = act.astype(jnp.bfloat16)
        put_taps(taps_ref, act, rows, cols)

    return fill


def back_means(sums, gain, pixels):
    channels = gain.shape[1]
    members = float(pixels * (channels // GROUPS))
    return group_mean(sums[0] * gain, members), group_mean(sums[1] * gain, members)


def column_total(partial):
    return jnp.sum(partial, axis=0, keepdims=True)


def weight_part(act_ref, narrow, lanes_ref, flip_ref, columns_ref, part_ref, cols):
    pixels, channels = act_ref.shape
    height = lax.axis_index("height")
    share = NARROW // 2
    flip_ref[...] = narrow.T
    own = pl.ds(pl.multiple_of((height % 2) * share, share), share)
    grad = flip_ref[own, :].astype(jnp.float32)
    column = lax.broadcasted_iota(jnp.int32, grad.shape, 1) & (cols - 1)
    for col_tap in range(3):
        shifted = grad
        if col_tap == 0:
            shifted = jnp.where(column == cols - 1, 0.0, pltpu.roll(grad, pixels - 1, 1))
        elif col_tap == 2:
            shifted = jnp.where(column == 0, 0.0, pltpu.roll(grad, 1, 1))
        for row_tap in range(3):
            tap = 3 * row_tap + col_tap
            place = slice(tap * share, (tap + 1) * share)
            if row_tap == 1:
                columns_ref[place, :] = shifted.astype(jnp.bfloat16)
                continue
            side, turn = (0, pixels - cols) if row_tap == 0 else (1, cols)
            masked = (shifted * lanes_ref[side : side + 1, :]).astype(jnp.bfloat16)
            columns_ref[place, :] = pltpu.roll(masked, turn, 1)
    part_ref[...] = jnp.dot(
        columns_ref[...], act_ref[...], preferred_element_type=jnp.float32
    ).astype(jnp.bfloat16)


def begin_back(read, weights_ref, mask_ref, taps_ref, total_ref, stop, cols):
    clear_edges(taps_ref, cols)

    def fill(rows):
        put_taps(taps_ref, read(rows), rows, cols)

    product = product_backward(weights_ref)
    begin_conv(taps_ref, product, total_ref, fill, lambda rows, part: part, cols)
    if stop:
        add_rows(taps_ref, product, mask_ref, total_ref, stop, cols)


def finish_back(
    weights_ref,
    mask_ref,
    taps_ref,
    total_ref,
    read,
    table_ref,
    which,
    cols,
    old_ref=None,
    pending=None,
):
    mean, inverse, gain, shift = norm_rows(table_ref, which)
    scale, offset = 0.5 * inverse * gain, 0.5 * shift
    sums = []

    def slope(rows, value):
        centered = read(rows) - mean
        half = centered * scale + offset
        turn = jnp.tanh(half)
        double = value * ((1.0 + turn) * (1.0 + half * (1.0 - turn)))
        sums.append((fold(double), fold(double * centered)))
        return double

    product = product_backward(weights_ref)
    end_conv(taps_ref, product, mask_ref, total_ref, slope, cols, old_ref, pending)
    plain, cross = sum(pair[0] for pair in sums), sum(pair[1] for pair in sums)
    return 0.5 * plain, 0.5 * inverse * cross


def norm_back(total_ref, double, sums, read, table_ref, which, pixels, scales_ref=None):
    mean, inverse, gain, shift = norm_rows(table_ref, which)
    mean_grad, mean_cross = back_means(sums, gain, pixels)
    slope = inverse * gain * (0.5 if double else 1.0)
    level, tilt = inverse * mean_grad, inverse * inverse * mean_cross
    if scales_ref is not None:
        for row, scales in enumerate((mean, slope, level, tilt)):
            scales_ref[row : row + 1, :] = scales

    def back(rows, inner):
        return total_ref[inner, :] * slope - level - (read(rows) - mean) * tilt

    return back


def own_lanes():
    block = lax.axis_index("height") // 2
    return pl.ds(pl.multiple_of(block * NARROW, NARROW), NARROW)


def narrow_back(total_ref, value_ref, scales_ref):
    lanes = own_lanes()
    mean, slope, level, tilt = (scales_ref[row : row + 1, lanes] for row in range(4))
    return total_ref[:, lanes] * slope - level - (value_ref[:, lanes] - mean) * tilt


def scaled_back(total_ref, value_ref, scales_ref, rows, inner):
    mean, slope, level, tilt = (scales_ref[row : row + 1, :] for row in range(4))
    return total_ref[inner, :] * slope - level - (value_ref[rows, :].astype(jnp.float32) - mean) * tilt


def turn_kernel(
    grad_ref,
    total_three_ref,
    scales_ref,
    residual_ref,
    mask_ref,
    weights_ref,
    old_sums_ref,
    total_ref,
    taps_ref,
    sums_ref,
    *,
    cols,
):
    grad_sums = []

    def read(rows):
        grad = scaled_back(total_three_ref, residual_ref, scales_ref, rows, rows)
        grad = grad_ref[rows, :].astype(jnp.float32) + grad
        grad = grad.astype(jnp.bfloat16).astype(jnp.float32)
        grad_sums.append(fold(grad))
        return grad

    begin_back(read, weights_ref.at[1], mask_ref, taps_ref, total_ref, EARLY_ROWS, cols)
    sums_ref[...] = old_sums_ref[...]
    sums_ref[7:8, :] = column_total(sum(grad_sums))


def norm_rows(table_ref, which):
    picks = (2 * which, 2 * which + 1, 6 + which, 9 + which)
    return tuple(table_ref[pick : pick + 1, :] for pick in picks)


def build_masks(ids_ref, mask_ref, lanes_ref, id_rows_ref, id_cols_ref, cols):
    rows = ids_ref.shape[1]

    def one_row(row, carry):
        here = ids_ref[0, row]
        place = pl.ds(pl.multiple_of(row * cols, cols), cols)
        id_rows_ref[place, :] = jnp.full((cols, LANES), here, jnp.int32)
        for side, other in ((0, row - 1), (1, row + 1)):
            inside = jnp.logical_and(other >= 0, other < rows)
            other_id = ids_ref[0, jnp.clip(other, 0, rows - 1)]
            same = jnp.where(jnp.logical_and(inside, other_id == here), 1.0, 0.0)
            mask_ref[side, place, :] = jnp.full((cols, LANES), same, jnp.float32)
        return carry

    lax.fori_loop(0, rows, one_row, 0)
    lane = lax.broadcasted_iota(jnp.int32, (8, LANES), 1)
    each = LANES // cols
    for block in range(rows // each):
        ids = jnp.full((8, LANES), ids_ref[0, block * each], jnp.int32)
        for step in range(1, each):
            ids = jnp.where(lane >= step * cols, ids_ref[0, block * each + step], ids)
        id_cols_ref[:, block * LANES : (block + 1) * LANES] = ids
    ids = id_cols_ref[...].astype(jnp.float32)
    pixels = ids.shape[1]
    pixel = lax.broadcasted_iota(jnp.int32, ids.shape, 1)
    above = jnp.where(pixel < cols, -1.0, pltpu.roll(ids, cols, 1))
    below = jnp.where(pixel >= pixels - cols, -1.0, pltpu.roll(ids, pixels - cols, 1))
    lanes_ref[0:1, :] = jnp.where(above == ids, 1.0, 0.0)[0:1]
    lanes_ref[1:2, :] = jnp.where(below == ids, 1.0, 0.0)[0:1]


def hold_kernel(
    ids_hbm,
    gains_hbm,
    shifts_hbm,
    biases_hbm,
    weights_hbm,
    qkv_hbm,
    proj_hbm,
    qv_bias_hbm,
    proj_bias_hbm,
    weights_ref,
    turned_ref,
    qkv_ref,
    proj_ref,
    table_ref,
    mask_ref,
    lanes_ref,
    id_rows_ref,
    id_cols_ref,
    ids_ref,
    gains_ref,
    shifts_ref,
    biases_ref,
    qv_bias_ref,
    proj_bias_ref,
    sems,
    *,
    cols,
):
    channels = weights_ref.shape[-1]
    small = [
        (ids_hbm, ids_ref),
        (gains_hbm, gains_ref),
        (shifts_hbm, shifts_ref),
        (biases_hbm, biases_ref),
        (qv_bias_hbm, qv_bias_ref),
        (proj_bias_hbm, proj_bias_ref),
    ]
    large = [(weights_hbm, weights_ref), (qkv_hbm, qkv_ref), (proj_hbm, proj_ref)]
    for which in range(2):
        for row_tap in range(3):
            for col_tap in range(3):
                place = slice(col_tap * channels, (col_tap + 1) * channels)
                large.append(
                    (
                        weights_hbm.at[which, 2 - row_tap, 2 - col_tap],
                        turned_ref.at[which, row_tap, :, place],
                    )
                )
    copies = [
        pltpu.make_async_copy(source, target, sems.at[index])
        for index, (source, target) in enumerate(small + large)
    ]
    for copy in copies:
        copy.start()
    for copy in copies[: len(small)]:
        copy.wait()
    build_masks(ids_ref, mask_ref, lanes_ref, id_rows_ref, id_cols_ref, cols)
    table_ref[6:9, :] = gains_ref[...]
    table_ref[9:12, :] = shifts_ref[...]
    table_ref[12:14, :] = biases_ref[...]
    table_ref[14:16, :] = qv_bias_ref[...]
    table_ref[16:17, :] = proj_bias_ref[...]
    for copy in copies[len(small) :]:
        copy.wait()


def conv_kernel(*refs, cols, count):
    pieces, refs = refs[:count], refs[count:]
    (
        weights_ref,
        params_ref,
        mask_ref,
        features_ref,
        act_one_ref,
        middle_ref,
        act_two_ref,
        residual_ref,
        table_ref,
        own_ref,
        taps_ref,
        sem,
    ) = refs
    pixels, channels = features_ref.shape
    wide = jnp.float32
    own_copy = pltpu.make_async_copy(pieces[0], own_ref, sem)
    own_copy.start()
    table_ref[...] = params_ref[...]
    clear_edges(taps_ref, cols)

    def read_input(rows):
        return features_ref[rows, :].astype(wide)

    def read_middle(rows):
        return middle_ref[rows, :]

    height = lax.axis_index("height")
    own_pixels = pixels // count
    seen = RunningStats(channels)
    for place in list(range(1, count)) + [0]:
        if place == 0:
            own_copy.wait()
        piece = (pieces[place] if place else own_ref)[0:own_pixels, :]
        start = pl.multiple_of((height ^ place) * own_pixels, own_pixels)
        features_ref[pl.ds(start, own_pixels), :] = piece
        seen.add(piece.astype(wide))
    table_ref[0:1, :], table_ref[1:2, :] = seen.finish(pixels)
    seen = RunningStats(channels)

    def keep(rows, value):
        seen.add(value)
        return value

    run_conv(
        taps_ref,
        product_forward(weights_ref.at[0]),
        mask_ref,
        middle_ref,
        activation(read_input, *norm_rows(table_ref, 0), act_one_ref, taps_ref, cols),
        lambda rows, part: part + table_ref[12:13, :],
        keep,
        cols,
    )
    table_ref[2:3, :], table_ref[3:4, :] = seen.finish(pixels)
    seen = RunningStats(channels)
    run_conv(
        taps_ref,
        product_forward(weights_ref.at[1]),
        mask_ref,
        residual_ref,
        activation(read_middle, *norm_rows(table_ref, 1), act_two_ref, taps_ref, cols),
        lambda rows, part: part + (read_input(rows) + table_ref[13:14, :]),
        keep,
        cols,
    )
    table_ref[4:5, :], table_ref[5:6, :] = seen.finish(pixels)


def score_kernel(
    qkv_ref,
    proj_ref,
    residual_ref,
    table_ref,
    id_rows_ref,
    id_cols_ref,
    flip_ref,
    query_ref,
    key_flip_ref,
    value_ref,
    soft_ref,
    out_flip_ref,
    output_ref,
    normed_ref,
    key_ref,
    value_flip_ref,
    *scores_refs,
    score_scale,
):
    pixels, channels = residual_ref.shape
    own_pixels = output_ref.shape[0]
    wide = jnp.float32
    exponent = score_scale * 1.4426950408889634
    mean, inverse, gain, shift = norm_rows(table_ref, 2)
    scale = inverse * gain

    def normalise(start):
        rows = slice(start, start + KEY_ROWS)
        normed = (residual_ref[rows, :] - mean) * scale + shift
        normed_ref[rows, :] = normed.astype(jnp.bfloat16)

    def project(start):
        rows = slice(start, start + KEY_ROWS)
        normed = normed_ref[rows, :]
        query_ref[rows, :] = (
            jnp.dot(normed, qkv_ref[:, 0:channels], preferred_element_type=wide)
            + table_ref[14:15, :]
        ).astype(jnp.bfloat16)
        keys = jnp.dot(
            normed, qkv_ref[:, channels : 2 * channels], preferred_element_type=wide
        ).astype(jnp.bfloat16)
        key_ref[rows, :] = keys
        key_flip_ref[:, rows] = keys.T
        values = (
            jnp.dot(normed, qkv_ref[:, 2 * channels :], preferred_element_type=wide)
            + table_ref[15:16, :]
        ).astype(jnp.bfloat16)
        value_ref[rows, :] = values
        value_flip_ref[:, rows] = values.T

    normalise(0)
    for start in range(0, pixels, KEY_ROWS):
        if start + KEY_ROWS < pixels:
            normalise(start + KEY_ROWS)
        project(start)
    quarter = flip_ref.shape[0]
    lanes = pl.ds(pl.multiple_of(own_quarter() * quarter, quarter), quarter)
    flip_ref[...] = normed_ref[:, lanes].T
    block = scores_refs[0].shape[1]
    steps = range(0, pixels, KEY_ROWS)

    def score(index):
        rows = slice(index * block, (index + 1) * block)
        for start in steps:
            keys = slice(start, start + KEY_ROWS)
            scores = lax.dot_general(
                key_ref[keys, :],
                query_ref[rows, :],
                (((1,), (1,)), ((), ())),
                preferred_element_type=wide,
            )
            same = widen(id_rows_ref[keys, :], block) == id_cols_ref[0:1, rows]
            scores_refs[index][keys, :] = jnp.where(same, scores, masked_score)

    def soften(index):
        rows = slice(index * block, (index + 1) * block)
        scores_ref = scores_refs[index]
        peak = jnp.full((8, block), masked_score, wide)
        for start in steps:
            scores = scores_ref[start : start + KEY_ROWS, :]
            peak = jnp.maximum(peak, jnp.max(scores.reshape(-1, 8, block), axis=0))
        peak = jnp.max(peak, axis=0, keepdims=True)
        total = jnp.zeros((8, block), wide)
        for start in steps:
            keys = slice(start, start + KEY_ROWS)
            powers = jnp.exp2((scores_ref[keys, :] - peak) * exponent)
            scores_ref[keys, :] = powers
            total = total + fold(powers)
        share = 1.0 / column_total(total)
        for start in steps:
            keys = slice(start, start + KEY_ROWS)
            soft_ref[keys, rows] = (scores_ref[keys, :] * share).astype(jnp.bfloat16)

    score(0)
    for index in range(len(scores_refs)):
        if index + 1 < len(scores_refs):
            score(index + 1)
        soften(index)
        rows = slice(index * block, (index + 1) * block)
        out_flip_ref[:, rows] = jnp.dot(
            value_flip_ref[...], soft_ref[:, rows], preferred_element_type=wide
        ).astype(jnp.bfloat16)
    height = lax.axis_index("height")
    own = pl.ds(pl.multiple_of(height * own_pixels, own_pixels), own_pixels)
    output_ref[...] = (
        residual_ref[own, :]
        + lax.dot_general(
            out_flip_ref[:, own],
            proj_ref[...],
            (((0,), (0,)), ((), ())),
            preferred_element_type=wide,
        )
        + table_ref[16:17, :]
    ).astype(jnp.bfloat16)


def own_quarter():
    height = lax.axis_index("height")
    return (height & 1) * 2 + ((height >> 1) & 1)


def attention_kernel(
    proj_ref,
    flip_ref,
    query_ref,
    key_flip_ref,
    value_ref,
    soft_ref,
    out_flip_ref,
    *refs,
    score_scale,
    count,
):
    pieces, (grad_ref, packed_ref, sums_ref), refs = (
        refs[:count],
        refs[count : count + 3],
        refs[count + 3 :],
    )
    pixels, channels = query_ref.shape
    blocks = pixels // SCORE_ROWS
    grads_refs, refs = refs[-blocks:], refs[:-blocks]
    *mixed_refs, mixed_ref, back_ref, score_grad_ref = refs
    wide = jnp.float32
    height = lax.axis_index("height")
    own_pixels = pixels // count
    for place, piece in enumerate(pieces):
        start = pl.multiple_of((height ^ place) * own_pixels, own_pixels)
        last = piece.shape[0]
        grad_ref[pl.ds(start, own_pixels), :] = piece[last - own_pixels : last, :]
    quarter = channels // 4
    own = pl.ds(pl.multiple_of(own_quarter() * quarter, quarter), quarter)
    block, count = SCORE_ROWS, blocks
    steps = range(0, pixels, KEY_ROWS)

    def block_rows(index):
        return slice(index * block, (index + 1) * block)

    for start in range(0, pixels, 2 * block):
        rows = slice(start, start + 2 * block)
        back_ref[rows, :] = lax.dot_general(
            grad_ref[rows, :],
            proj_ref[...],
            (((1,), (1,)), ((), ())),
            preferred_element_type=wide,
        ).astype(jnp.bfloat16)

    def weigh(index):
        total = jnp.zeros((8, block), wide)
        for start in steps:
            keys = slice(start, start + KEY_ROWS)
            weight_grad = lax.dot_general(
                value_ref[keys, :],
                back_ref[block_rows(index), :],
                (((1,), (1,)), ((), ())),
                preferred_element_type=wide,
            )
            grads_refs[index][keys, :] = weight_grad
            total = total + fold(soft_ref[keys, block_rows(index)].astype(wide) * weight_grad)
        return column_total(total)

    def slope(index, dots):
        for start in steps:
            keys = slice(start, start + KEY_ROWS)
            weights = soft_ref[keys, block_rows(index)].astype(wide)
            score_grad_ref[keys, block_rows(index)] = (
                weights * (grads_refs[index][keys, :] - dots)
            ).astype(jnp.bfloat16)

    dots = weigh(0)
    for index in range(count):
        now, rows = dots, block_rows(index)
        if index + 1 < count:
            dots = weigh(index + 1)
        slope(index, now)
        packed_ref[rows, 2 * channels :] = jnp.dot(
            soft_ref[rows, :], back_ref[...], preferred_element_type=wide
        ).astype(jnp.bfloat16)
        query_grad = jnp.dot(
            key_flip_ref[...], score_grad_ref[:, rows], preferred_element_type=wide
        )
        packed_ref[rows, 0:channels] = (query_grad * score_scale).astype(jnp.bfloat16).T
    for start in range(0, pixels, 2 * block):
        rows = slice(start, start + 2 * block)
        packed_ref[rows, channels : 2 * channels] = (
            jnp.dot(score_grad_ref[rows, :], query_ref[...], preferred_element_type=wide)
            * score_scale
        ).astype(jnp.bfloat16)

    def pack(rows, carry):
        return (
            carry[0] + fold(packed_ref[rows, 0:channels].astype(wide)),
            carry[1] + fold(packed_ref[rows, 2 * channels :].astype(wide)),
            carry[2] + fold(grad_ref[rows, :].astype(wide)),
        )

    zeros = jnp.zeros((8, channels), wide)
    totals = zeros, zeros, zeros
    for start in range(0, pixels, CHUNK):
        totals = pack(pl.ds(start, CHUNK), totals)
    sums_ref[...] = jnp.zeros(sums_ref.shape, wide)
    for row, total in enumerate(totals):
        sums_ref[8 + row : 9 + row, :] = column_total(total)
    mixed_ref[:, 0 : 3 * channels] = jnp.dot(
        flip_ref[...], packed_ref[...], preferred_element_type=wide
    ).astype(jnp.bfloat16)
    mixed_ref[:, 3 * channels :] = jnp.dot(
        out_flip_ref[own, :], grad_ref[...], preferred_element_type=wide
    ).astype(jnp.bfloat16)
    share = quarter // len(mixed_refs)
    me = lax.axis_index("canvas")
    for step, target in enumerate(mixed_refs):
        target[...] = mixed_ref[pl.ds(pl.multiple_of((me ^ step) * share, share), share), :]


def third_kernel(
    qkv_ref,
    grad_ref,
    packed_ref,
    residual_ref,
    table_ref,
    act_two_ref,
    lanes_ref,
    old_sums_ref,
    total_ref,
    scales_ref,
    sums_ref,
    part_ref,
    flip_ref,
    columns_ref,
    *,
    cols,
):
    pixels, channels = residual_ref.shape
    block = 2 * FILL_ROWS
    wide = jnp.float32
    mean, inverse, gain, shift = norm_rows(table_ref, 2)
    zeros = jnp.zeros((8, channels), wide)

    sums = (zeros, zeros)
    for start in range(0, pixels, block):
        rows = pl.ds(start, block)
        normed_grad = lax.dot_general(
            packed_ref[rows, :], qkv_ref[...], (((1,), (1,)), ((), ())), preferred_element_type=wide
        )
        total_ref[rows, :] = normed_grad
        centered = residual_ref[rows, :] - mean
        sums = sums[0] + fold(normed_grad), sums[1] + fold(normed_grad * centered)
    sums = sums[0], sums[1] * inverse
    sums_ref[...] = old_sums_ref[...]
    sums_ref[5:6, :] = column_total(sums[1])
    sums_ref[6:7, :] = column_total(sums[0])
    norm_back(
        total_ref, False, sums, lambda rows: residual_ref[rows, :], table_ref, 2, pixels, scales_ref
    )
    narrow = narrow_back(total_ref, residual_ref, scales_ref)
    narrow = (grad_ref[:, own_lanes()].astype(wide) + narrow).astype(jnp.bfloat16)
    weight_part(act_two_ref, narrow, lanes_ref, flip_ref, columns_ref, part_ref, cols)


def second_kernel(
    old_total_ref,
    taps_ref,
    middle_ref,
    table_ref,
    act_one_ref,
    mask_ref,
    lanes_ref,
    weights_ref,
    old_sums_ref,
    part_two_ref,
    total_ref,
    scales_ref,
    sums_ref,
    keep_one_ref,
    send_one_ref,
    keep_two_ref,
    send_two_ref,
    flip_ref,
    columns_ref,
    part_ref,
    *,
    cols,
):
    pixels, channels = middle_ref.shape

    def read(rows):
        return middle_ref[rows, :]

    sums = finish_back(
        weights_ref.at[1],
        mask_ref,
        taps_ref,
        total_ref,
        read,
        table_ref,
        1,
        cols,
        old_total_ref,
        EARLY_ROWS,
    )
    norm_back(total_ref, True, sums, read, table_ref, 1, pixels, scales_ref)
    narrow = narrow_back(total_ref, middle_ref, scales_ref).astype(jnp.bfloat16)
    weight_part(act_one_ref, narrow, lanes_ref, flip_ref, columns_ref, part_ref, cols)
    sums_ref[...] = old_sums_ref[...]
    sums_ref[2:3, :] = column_total(sums[1])
    sums_ref[3:4, :] = column_total(sums[0])
    keep_half(part_ref, keep_one_ref, send_one_ref)
    keep_half(part_two_ref, keep_two_ref, send_two_ref)


def near_far():
    core = lax.axis_index("height") & 1
    return 1 + core, 2 - core


def keep_half(source_ref, keep_ref, send_ref):
    me = lax.axis_index("canvas")
    near, far = near_far()
    rows, width = keep_ref.shape[0] // 2, keep_ref.shape[1]
    for target_ref, flip in ((keep_ref, 0), (send_ref, near)):
        for slot, other in enumerate((0, far)):
            place = pl.ds(pl.multiple_of((me ^ flip ^ other) * width, width), width)
            target_ref[slot * rows : (slot + 1) * rows, :] = source_ref[:, place]


def first_kernel(
    total_two_ref,
    scales_ref,
    middle_ref,
    features_ref,
    table_ref,
    mask_ref,
    old_sums_ref,
    weights_ref,
    own_ref,
    sums_ref,
    partial_ref,
    total_ref,
    taps_ref,
    *,
    cols,
):
    def read(rows):
        return features_ref[rows, :].astype(jnp.float32)

    grad_sums = []

    def read_grad(rows):
        grad = scaled_back(total_two_ref, middle_ref, scales_ref, rows, rows)
        grad = grad.astype(jnp.bfloat16).astype(jnp.float32)
        grad_sums.append(fold(grad))
        return grad

    weights = weights_ref.at[0]
    begin_back(read_grad, weights, mask_ref, taps_ref, total_ref, total_ref.shape[0], cols)
    sums = finish_back(weights, mask_ref, taps_ref, total_ref, read, table_ref, 0, cols)
    partial_ref[0:8, :], partial_ref[8:16, :] = sums
    sums_ref[...] = old_sums_ref[...]
    sums_ref[0:1, :] = column_total(sums[1])
    sums_ref[1:2, :] = column_total(sums[0])
    sums_ref[4:5, :] = column_total(sum(grad_sums))
    count = own_ref.shape[0]
    own = pl.ds(pl.multiple_of(lax.axis_index("height") * count, count), count)
    own_ref[...] = total_ref[own, :]


def own_kernel(
    own_ref,
    partial_ref,
    features_ref,
    grad_ref,
    total_three_ref,
    residual_ref,
    scales_ref,
    table_ref,
    input_grad_ref,
):
    def read(rows):
        return features_ref[rows, :].astype(jnp.float32)

    sums = partial_ref[0:8, :], partial_ref[8:16, :]
    pixels = features_ref.shape[0]
    back = norm_back(own_ref, True, sums, read, table_ref, 0, pixels)
    count = own_ref.shape[0]
    own = pl.ds(pl.multiple_of(lax.axis_index("height") * count, count), count)
    total = scaled_back(total_three_ref, residual_ref, scales_ref, own, own)
    total = grad_ref[own, :].astype(jnp.float32) + total
    input_grad_ref[...] = (total + back(own, slice(0, count))).astype(jnp.bfloat16)


def place_kernel(*refs):
    joints, packed_ref = refs[:-1], refs[-1]
    share = packed_ref.shape[0] // len(joints)
    me = lax.axis_index("canvas")
    for step, joint in enumerate(joints):
        place = pl.ds(pl.multiple_of((me ^ step) * share, share), share)
        packed_ref[place, :] = joint[...]


def cut_kernel(packed_ref, *half_refs):
    rows = half_refs[0].shape[0]
    for index, half_ref in enumerate(half_refs):
        half_ref[...] = packed_ref[index * rows : (index + 1) * rows, :]


def spread_quarters(packed, flips, qkv_ref, proj_ref, qkv_hbm, proj_hbm, sems):
    quarter = packed[0].shape[0]
    inner = qkv_ref.shape[2]
    copies = []
    for index, packed_ref in enumerate(packed):
        owner = own_quarter() ^ flips[index]
        rows = pl.ds(pl.multiple_of(owner * quarter, quarter), quarter)
        qkv_ref[index] = packed_ref[:, 0:inner].astype(jnp.float32)
        proj_ref[index] = packed_ref[:, inner:].astype(jnp.float32)
        for which, (held, target) in enumerate(((qkv_ref, qkv_hbm), (proj_ref, proj_hbm))):
            copy = pltpu.make_async_copy(held.at[index], target.at[rows, :], sems.at[index, which])
            copy.start()
            copies.append(copy)
    return copies


def join_kernel(*refs):
    packed, (qkv_hbm, proj_hbm, qkv_ref, proj_ref, sems) = refs[:-5], refs[-5:]
    copies = spread_quarters(packed, [0, 2], qkv_ref, proj_ref, qkv_hbm, proj_hbm, sems)
    for copy in copies:
        copy.wait()


def halve_kernel(keep_ref, got_ref, hold_ref, send_ref):
    total = keep_ref[...].astype(jnp.float32) + got_ref[...].astype(jnp.float32)
    rows = hold_ref.shape[0]
    hold_ref[...] = total[0:rows]
    send_ref[0:rows, :] = total[rows:].astype(jnp.bfloat16)


def halve_both_kernel(
    keep_ref, got_ref, keep_two_ref, got_two_ref, hold_ref, send_ref, hold_two_ref
):
    rows = hold_ref.shape[0]
    halve_kernel(keep_ref, got_ref, hold_ref, send_ref)
    halve_kernel(keep_two_ref, got_two_ref, hold_two_ref, send_ref.at[rows : 2 * rows, :])


def last_kernel(
    chip_ref,
    both_a_ref,
    both_b_ref,
    old_qkv,
    old_proj,
    qkv_hbm,
    proj_hbm,
    qkv_ref,
    proj_ref,
    sems,
):
    copies = []
    rows = both_a_ref.shape[0]
    inner = qkv_ref.shape[2]
    chips = (chip_ref.at[0:rows, :], chip_ref.at[rows : 2 * rows, :])
    for index, piece_ref in enumerate((*chips, both_a_ref, both_b_ref)):
        start = ((own_quarter() ^ (1 if index < 2 else 3)) * 2 + index % 2) * rows
        target = pl.ds(pl.multiple_of(start, rows), rows)
        qkv_ref[index] = piece_ref[:, 0:inner].astype(jnp.float32)
        proj_ref[index] = piece_ref[:, inner:].astype(jnp.float32)
        for which, (held, whole) in enumerate(((qkv_ref, qkv_hbm), (proj_ref, proj_hbm))):
            copy = pltpu.make_async_copy(held.at[index], whole.at[target, :], sems.at[index, which])
            copy.start()
            copies.append(copy)
    for copy in copies:
        copy.wait()


def sums_kernel(
    sums_ref,
    got_sums_ref,
    hold_one_ref,
    hold_two_ref,
    got_ref,
    share_ref,
    gains_ref,
    shifts_ref,
    conv_ref,
    qv_ref,
    bias_ref,
):
    rows = hold_one_ref.shape[0]
    for which, hold_ref in enumerate((hold_one_ref, hold_two_ref)):
        got = got_ref[which * rows : (which + 1) * rows, :].astype(jnp.float32)
        share_ref[which] = (hold_ref[...] + got).reshape(share_ref.shape[1:])
    total = sums_ref[...] + got_sums_ref[...]
    for row, start in enumerate((0, 2, 5)):
        gains_ref[row : row + 1, :] = total[start : start + 1]
        shifts_ref[row : row + 1, :] = total[start + 1 : start + 2]
    conv_ref[0:1, :] = total[4:5]
    conv_ref[1:2, :] = total[7:8]
    qv_ref[...] = total[8:10]
    bias_ref[...] = total[10:11]


def call_kernel(kernel, outputs, scratch, operands, places, flops, limit, out_places=None, aliases={}):
    out_places = out_places or "v" * len(outputs)
    spaces = {
        "v": pl.BlockSpec(memory_space=pltpu.VMEM),
        "s": pl.BlockSpec(memory_space=pltpu.SMEM),
        "h": pl.BlockSpec(memory_space=pl.ANY),
        "o": pl.BlockSpec(memory_space=pltpu.VMEM),
        "a": pl.BlockSpec(memory_space=pl.ANY),
    }
    moved = 8 * flops // LANES
    held = {"v": pltpu.VMEM, "h": pltpu.HBM, "o": jax.ShapeDtypeStruct}
    operands = [
        pltpu.with_memory_space_constraint(array, pltpu.HBM) if place == "h" else array
        for array, place in zip(operands, places)
    ]
    return pl.pallas_call(
        kernel,
        out_shape=[held[place](*output) for output, place in zip(outputs, out_places)],
        in_specs=[spaces[place] for place in places],
        out_specs=[spaces[place] for place in out_places],
        scratch_shapes=scratch,
        input_output_aliases=aliases,
        compiler_params=pltpu.CompilerParams(vmem_limit_bytes=limit * 2**20),
        cost_estimate=pl.CostEstimate(flops=flops, bytes_accessed=moved, transcendentals=0),
    )(*operands)


def send_height(block, step):
    size = lax.axis_size("height")
    return lax.ppermute(block, "height", [(i, i ^ step) for i in range(size)])


def with_cores(blocks, other):
    pieces = [blocks[0], other]
    for block in blocks[1:]:
        pieces += [block, send_height(block, 1)]
    return pieces


def send_canvas(block, step):
    size = lax.axis_size("canvas")
    return lax.ppermute(block, "canvas", [(i, i ^ step) for i in range(size)])


def send_phase(block, phase):
    canvases, size = lax.axis_size("canvas"), lax.axis_size("height")
    pairs = []
    for canvas in range(canvases):
        for height in range(size):
            step = 2 if (height ^ phase) & 1 else 1
            pairs.append((canvas * size + height, (canvas ^ step) * size + height))
    return lax.ppermute(block, ("canvas", "height"), pairs)


def trade_canvas(pieces):
    return [pieces[0]] + [send_canvas(piece, step) for step, piece in enumerate(pieces) if step]


def whole_canvas(
    features,
    tile_ids,
    norm_gains,
    norm_shifts,
    conv_weights,
    conv_biases,
    qkv_weight,
    qv_bias,
    proj_weight,
    proj_bias,
    cotangent,
):
    height_size = lax.axis_size("height")
    canvas_size = lax.axis_size("canvas")
    local_rows, cols, channels = features.shape[1:]
    all_rows = tile_ids.shape[1]
    pixels = all_rows * cols
    own_pixels = local_rows * cols
    out_share = channels // height_size
    ci_share = channels // canvas_size
    quarter = channels // 4
    row_share = quarter // canvas_size
    low, wide = jnp.bfloat16, jnp.float32

    own_features = features.reshape(own_pixels, channels)
    own_grad = cotangent.reshape(own_pixels, channels)
    steps = range(2, height_size, 2)
    held_features = [own_features] + [send_height(own_features, step) for step in steps]
    plane = ((pixels, channels), low)
    plane_wide = ((pixels, channels), wide)
    sums_shape = ((16, channels), wide)
    mixed_shapes = [((row_share, 4 * channels), low)] * canvas_size
    taps = pltpu.VMEM((pixels + 2 * cols, 3 * channels), low)
    held_wide = pltpu.VMEM((pixels, channels), wide)
    flipped = pltpu.VMEM((channels, pixels), low)
    narrow = pltpu.VMEM((NARROW, pixels), low)
    columns = pltpu.VMEM((9 * out_share, pixels), low)
    part_held = pltpu.VMEM((9 * out_share, channels), low)
    sem = pltpu.SemaphoreType.DMA
    conv_flops = 2 * 9 * pixels * channels * channels
    dot_flops = 2 * pixels * channels * channels
    score_flops = 2 * pixels * pixels * channels
    scale = channels ** (-0.5)

    (
        held_conv,
        turned,
        held_qkv,
        held_proj,
        params,
        mask,
        lane_mask,
        id_rows,
        id_cols,
    ) = call_kernel(
        functools.partial(hold_kernel, cols=cols),
        [
            (conv_weights.shape, low),
            ((2, 3, channels, 3 * channels), low),
            (qkv_weight.shape, low),
            (proj_weight.shape, low),
            ((24, channels), wide),
            ((2, pixels, LANES), wide),
            ((8, pixels), wide),
            ((pixels, LANES), jnp.int32),
            ((8, pixels), jnp.int32),
        ],
        [
            pltpu.SMEM(tile_ids.shape, jnp.int32),
            pltpu.VMEM(norm_gains.shape, wide),
            pltpu.VMEM(norm_shifts.shape, wide),
            pltpu.VMEM(conv_biases.shape, wide),
            pltpu.VMEM(qv_bias.shape, wide),
            pltpu.VMEM((1, channels), wide),
            sem((27,)),
        ],
        [
            tile_ids,
            norm_gains,
            norm_shifts,
            conv_biases,
            conv_weights,
            qkv_weight,
            proj_weight,
            qv_bias,
            proj_bias.reshape(1, channels),
        ],
        "h" * 9,
        conv_flops,
        8,
    )
    held_features[1:] = [
        lax.optimization_barrier((params, block))[1] for block in held_features[1:]
    ]
    other_core = send_height(jnp.concatenate([own_features, own_grad], axis=0), 1)
    pieces = with_cores(held_features, other_core)
    far_grad, *pieces[4::2] = lax.optimization_barrier((own_grad, *held_features[2:]))
    held_grads = [own_grad, send_height(own_grad, 2)]
    held_grads[1], pieces[2] = lax.optimization_barrier((held_grads[1], held_features[1]))
    held_grads += [send_height(far_grad, step) for step in steps[1:]]

    all_features, act_one, middle, act_two, residual, table = call_kernel(
        functools.partial(conv_kernel, cols=cols, count=height_size),
        [plane, plane, plane_wide, plane, plane_wide, ((24, channels), wide)],
        [pltpu.VMEM((own_pixels, channels), low), taps, sem],
        [*pieces, held_conv, params, mask],
        "h" + "v" * (height_size + 2),
        2 * conv_flops,
        16,
    )
    residual, *held_grads = lax.optimization_barrier((residual, *held_grads))
    grad_pieces = with_cores(held_grads, other_core)
    normed_flip, query, key_flip, value, soft, out_flip, output = call_kernel(
        functools.partial(score_kernel, score_scale=scale),
        [
            ((quarter, pixels), low),
            plane,
            ((channels, pixels), low),
            plane,
            ((pixels, pixels), low),
            ((channels, pixels), low),
            ((own_pixels, channels), low),
        ],
        [
            pltpu.VMEM((pixels, channels), low),
            pltpu.VMEM((pixels, channels), low),
            flipped,
            *[pltpu.VMEM((pixels, SCORE_ROWS), wide)] * (pixels // SCORE_ROWS),
        ],
        [
            held_qkv,
            held_proj,
            residual,
            table,
            id_rows,
            id_cols,
        ],
        "vvvvvv",
        3 * dot_flops + 2 * score_flops,
        20,
        "v" * 6 + "o",
    )
    normed_flip, *grad_pieces = lax.optimization_barrier((normed_flip, *grad_pieces))
    all_grad, packed, sums, *mixed = call_kernel(
        functools.partial(attention_kernel, score_scale=scale, count=height_size),
        [plane, ((pixels, 3 * channels), low), sums_shape, *mixed_shapes],
        [
            pltpu.VMEM((quarter, 4 * channels), low),
            pltpu.VMEM((pixels, channels), low),
            pltpu.VMEM((pixels, pixels), low),
            *[pltpu.VMEM((pixels, SCORE_ROWS), wide)] * (pixels // SCORE_ROWS),
        ],
        [held_proj, normed_flip, query, key_flip, value, soft, out_flip, *grad_pieces],
        "v" * (7 + height_size),
        3 * dot_flops + 4 * score_flops,
        20,
    )
    mixed = trade_canvas(mixed)
    total_three, scales_three, sums, part_two = call_kernel(
        functools.partial(third_kernel, cols=cols),
        [plane_wide, ((8, channels), wide), sums_shape, ((9 * out_share, channels), low)],
        [narrow, columns],
        [held_qkv, all_grad, packed, residual, table, act_two, lane_mask, sums],
        "vvvvvvvv",
        3 * dot_flops + conv_flops // height_size,
        16,
    )
    half_total, half_taps, sums = call_kernel(
        functools.partial(turn_kernel, cols=cols),
        [plane_wide, (taps.shape, low), sums_shape],
        [],
        [all_grad, total_three, scales_three, residual, mask, turned, sums],
        "vvvvvvv",
        conv_flops // 2,
        16,
    )
    half_total, *mixed = lax.optimization_barrier((half_total, *mixed))
    mixed_sum = mixed[0].astype(wide)
    for piece in mixed[1:]:
        mixed_sum = mixed_sum + piece.astype(wide)
    mixed_sum = mixed_sum.astype(low)
    joints = trade_canvas([mixed_sum] * canvas_size)
    halves = [((2 * 9 * out_share, ci_share), low)] * 4
    total_two, scales, sums, keep_one, send_one, keep_two, send_two = call_kernel(
        functools.partial(second_kernel, cols=cols),
        [plane_wide, ((8, channels), wide), sums_shape, *halves],
        [narrow, columns, part_held],
        [half_total, half_taps, middle, table, act_one, mask, lane_mask, turned, sums, part_two],
        "v" * 10,
        conv_flops // 2,
        20,
    )
    total_two, *joints = lax.optimization_barrier((total_two, *joints))
    (own_mixed,) = call_kernel(
        place_kernel,
        [((quarter, 4 * channels), low)],
        [],
        joints,
        "v" * canvas_size,
        1,
        12,
    )
    own_mixed, send_one, send_two = lax.optimization_barrier((own_mixed, send_one, send_two))
    chip_mixed = send_height(own_mixed, 2)
    core_mixed = send_height(own_mixed, 1)
    got_one, got_two = send_phase(send_one, 0), send_phase(send_two, 0)
    own_total, sums, partial_sums = call_kernel(
        functools.partial(first_kernel, cols=cols),
        [((own_pixels, channels), wide), sums_shape, sums_shape],
        [held_wide, taps],
        [total_two, scales, middle, all_features, table, mask, sums, turned],
        "vvvvvvvv",
        1,
        20,
    )
    got_sums, own_sums = send_phase(sums, 0), sums
    sums, core_mixed, got_one, got_two = lax.optimization_barrier(
        (sums, core_mixed, got_one, got_two)
    )
    share_rows = 9 * out_share
    hold_one, send_share, hold_two = call_kernel(
        halve_both_kernel,
        [
            ((share_rows, ci_share), wide),
            ((2 * share_rows, ci_share), low),
            ((share_rows, ci_share), wide),
        ],
        [],
        [keep_one, got_one, keep_two, got_two],
        "vvvv",
        1,
        12,
    )
    got_share = send_phase(send_share, 1)

    def widened(count, rows):
        return [
            pltpu.VMEM((count, rows, 3 * channels), wide),
            pltpu.VMEM((count, rows, channels), wide),
            sem((count, 2)),
        ]

    grad_shapes = [(qkv_weight.shape, wide), (proj_weight.shape, wide)]
    core_mixed, hold_one = lax.optimization_barrier((core_mixed, hold_one))
    qkv_grad, proj_grad = call_kernel(
        join_kernel,
        grad_shapes,
        widened(2, quarter),
        [own_mixed, core_mixed],
        "vv",
        1,
        12,
        "hh",
    )
    qkv_grad, chip_mixed, got_sums = lax.optimization_barrier((qkv_grad, chip_mixed, got_sums))
    sums = own_sums + got_sums
    got_sums = send_phase(sums, 1)
    chip_halves = call_kernel(
        cut_kernel,
        [((quarter // 2, 4 * channels), low)] * 2,
        [],
        [chip_mixed],
        "v",
        1,
        12,
    )
    both_halves = [send_height(half, 1) for half in chip_halves]
    qkv_grad, proj_grad = call_kernel(
        last_kernel,
        grad_shapes,
        widened(4, quarter // 2),
        [chip_mixed, *both_halves, qkv_grad, proj_grad],
        "vvvhh",
        1,
        12,
        "hh",
        {3: 0, 4: 1},
    )
    qkv_grad, own_total = lax.optimization_barrier((qkv_grad, own_total))
    (input_grad,) = call_kernel(
        own_kernel,
        [((own_pixels, channels), low)],
        [],
        [
            own_total,
            partial_sums,
            all_features,
            all_grad,
            total_three,
            residual,
            scales_three,
            table,
        ],
        "v" * 8,
        dot_flops // 4,
        12,
        "o",
    )
    input_grad, got_share, got_sums = lax.optimization_barrier((input_grad, got_share, got_sums))
    vector_shapes = [norm_gains.shape, norm_shifts.shape, conv_biases.shape, qv_bias.shape]
    conv_grad, gains_grad, shifts_grad, biases_grad, qv_grad, proj_bias_grad = call_kernel(
        sums_kernel,
        [((2, 3, 3, out_share, ci_share), wide)]
        + [(shape, wide) for shape in vector_shapes + [(1, channels)]],
        [],
        [sums, got_sums, hold_one, hold_two, got_share],
        "vvvvv",
        1,
        12,
        "o" * 6,
    )
    own_shape = (1, local_rows, cols, channels)
    return (
        output.reshape(own_shape),
        input_grad.reshape(own_shape),
        gains_grad,
        shifts_grad,
        jnp.swapaxes(conv_grad, 3, 4),
        biases_grad,
        qkv_grad,
        qv_grad,
        proj_grad,
        proj_bias_grad.reshape(channels),
    )


def on_device(*arrays):
    features, tile_ids = arrays[0], arrays[1]
    local_rows, cols, channels = features.shape[1:]
    pixels = tile_ids.shape[1] * cols
    height_size, canvas_size = lax.axis_size("height"), lax.axis_size("canvas")
    powers = all(size & (size - 1) == 0 for size in (height_size, canvas_size, cols))
    fits = (
        powers
        and height_size > 2
        and canvas_size == 4
        and channels == LANES * canvas_size
        and pixels <= MOST_PIXELS
        and pixels % FILL_ROWS == 0
        and pixels >= EARLY_ROWS
        and FILL_ROWS % CHUNK == 0
        and pixels % SCORE_ROWS == 0
        and pixels % KEY_ROWS == 0
        and (local_rows * cols) % LANES == 0
        and CHUNK % cols == 0
        and cols % 16 == 0
        and channels % (LANES * canvas_size) == 0
        and 2 * channels == NARROW * height_size
    )
    return whole_canvas(*arrays) if fits else split_canvas(*arrays)


def solution(mesh):
    in_specs = (
        P("canvas", "height", None, None),
        P("canvas", None),
        P(),
        P(),
        P(),
        P(),
        P(),
        P(),
        P(),
        P(),
        P("canvas", "height", None, None),
    )
    out_specs = (
        P("canvas", "height", None, None),
        P("canvas", "height", None, None),
        P(),
        P(),
        P(None, None, None, "canvas", "height"),
        P(),
        P(),
        P(),
        P(),
        P(),
    )
    return jax.shard_map(
        on_device, mesh=mesh, in_specs=in_specs, out_specs=out_specs, check_vma=False
    )
```

```python
import functools

import jax
import jax.numpy as jnp
from jax import lax
from jax.experimental import pallas as pl
from jax.experimental.pallas import tpu as pltpu
from jax.sharding import PartitionSpec as P

GROUPS = 32


epsilon = 1e-06
masked_score = -1e30
MOST_PIXELS = 1024
LANES = 128
NARROW = 128
CHUNK = 128
FILL_ROWS = 256
EARLY_ROWS = 256
SCORE_ROWS = 256
KEY_ROWS = 256


def extended(block, sides, width):
    for axis, dim in sides:
        count = lax.axis_size(axis)
        forward = [(i, i + 1) for i in range(count - 1)]
        backward = [(target, source) for source, target in forward]
        low = lax.ppermute(
            lax.slice_in_dim(block, block.shape[dim] - width, None, axis=dim), axis, forward
        )
        high = lax.ppermute(lax.slice_in_dim(block, 0, width, axis=dim), axis, backward)
        block = jnp.concatenate([low, block, high], axis=dim)
    return block


def group_total(vector):
    return vector.reshape(GROUPS, -1).sum(axis=1)


def spread_groups(vector, channels):
    return jnp.repeat(vector, channels // GROUPS)


def norm_forward(values, gain, shift, members):
    channels = values.shape[1]
    totals = lax.psum(group_total(jnp.sum(values, axis=0)), "height")
    centered = values - spread_groups(totals / members, channels)
    squares = lax.psum(group_total(jnp.sum(centered * centered, axis=0)), "height")
    inverse = spread_groups(lax.rsqrt(squares / members + epsilon), channels)
    normed = centered * inverse
    return (normed, inverse, normed * gain + shift)


def norm_backward(grad_in, normed, inverse, gain, members):
    channels = grad_in.shape[1]
    scaled = grad_in * gain
    both_sums = lax.psum(
        (group_total(jnp.sum(scaled, axis=0)), group_total(jnp.sum(scaled * normed, axis=0))),
        "height",
    )
    mean_grad = spread_groups(both_sums[0] / members, channels)
    mean_cross = spread_groups(both_sums[1] / members, channels)
    result = inverse * (scaled - mean_grad - normed * mean_cross)
    return (result, jnp.sum(grad_in * normed, axis=0), jnp.sum(grad_in, axis=0))


def swish(values):
    return values * jax.nn.sigmoid(values)


def swish_slope(values):
    sigmoid_part = jax.nn.sigmoid(values)
    return sigmoid_part * (1.0 + values * (1.0 - sigmoid_part))


def tap_columns(padded, row_mask, local_rows, canvas_cols):
    pieces = []
    for row_tap in range(3):
        rows_taken = padded[row_tap : row_tap + local_rows] * row_mask[:, row_tap, None, None]
        for col_tap in range(3):
            pieces.append(rows_taken[:, col_tap : col_tap + canvas_cols])
    stacked = jnp.concatenate(pieces, axis=2)
    return stacked.reshape(local_rows * canvas_cols, stacked.shape[2])


def conv_forward(acts, row_mask, weight, bias):
    local_rows, canvas_cols, channels = acts.shape
    rimmed = extended(acts, (("height", 0),), 1)
    padded = jnp.pad(rimmed, ((0, 0), (1, 1), (0, 0)))
    gathered = tap_columns(padded, row_mask, local_rows, canvas_cols)
    result = (
        jnp.dot(
            gathered, weight.reshape(9 * channels, channels), preferred_element_type=jnp.float32
        )
        + bias
    )
    return (result, gathered)


def conv_backward(grad_low, row_mask, weight, gathered):
    local_rows, canvas_cols, channels = grad_low.shape
    flat_grad = grad_low.reshape(local_rows * canvas_cols, channels)
    weight_grad = lax.dot_general(
        gathered, flat_grad, (((0,), (0,)), ((), ())), preferred_element_type=jnp.float32
    )
    rimmed = extended(grad_low, (("height", 0),), 1)
    padded = jnp.pad(rimmed, ((0, 0), (1, 1), (0, 0)))
    grad_taps = tap_columns(padded, row_mask, local_rows, canvas_cols)
    flipped = jnp.transpose(weight[::-1, ::-1], (0, 1, 3, 2)).reshape(9 * channels, channels)
    input_part = jnp.dot(grad_taps, flipped, preferred_element_type=jnp.float32)
    return (
        input_part,
        weight_grad.reshape(3, 3, channels, channels),
        jnp.sum(flat_grad.astype(jnp.float32), axis=0),
    )


def take_rows(array, offset, count):
    return lax.dynamic_slice_in_dim(array, offset, count)


def score_grads(
    queries, out_grad, log_total, row_dots, query_ids, key_rows, value_rows, key_ids, score_scale
):
    scores = (
        lax.dot_general(
            queries, key_rows, (((1,), (1,)), ((), ())), preferred_element_type=jnp.float32
        )
        * score_scale
    )
    same_tile = query_ids[:, None] == key_ids[None, :]
    softmax_block = jnp.exp(jnp.where(same_tile, scores - log_total[:, None], masked_score))
    weight_grad = lax.dot_general(
        out_grad, value_rows, (((1,), (1,)), ((), ())), preferred_element_type=jnp.float32
    )
    score_grad = (softmax_block * (weight_grad - row_dots[:, None])).astype(jnp.bfloat16)
    return (softmax_block.astype(jnp.bfloat16), score_grad)


def split_canvas(
    features,
    tile_ids,
    norm_gains,
    norm_shifts,
    conv_weights,
    conv_biases,
    qkv_weight,
    qv_bias,
    proj_weight,
    proj_bias,
    cotangent,
):
    height_size = lax.axis_size("height")
    local_rows = features.shape[1]
    canvas_cols = features.shape[2]
    channels = features.shape[3]
    pixels = local_rows * canvas_cols
    row_ids = tile_ids[0]
    all_rows = row_ids.shape[0]
    members = float(all_rows * canvas_cols * (channels // GROUPS))
    score_scale = channels ** (-0.5)
    first_row = lax.axis_index("height") * local_rows
    edge_ids = jnp.full((1,), -1, jnp.int32)
    padded_ids = jnp.concatenate([edge_ids, row_ids, edge_ids])
    near_ids = lax.dynamic_slice_in_dim(padded_ids, first_row, local_rows + 2)
    own_rows = near_ids[1 : local_rows + 1]
    row_mask = jnp.stack(
        [near_ids[row_tap : row_tap + local_rows] == own_rows for row_tap in range(3)], axis=1
    ).astype(jnp.bfloat16)
    key_ids = jnp.repeat(row_ids, canvas_cols)
    query_ids = jnp.repeat(own_rows, canvas_cols)
    grid_shape = (local_rows, canvas_cols, channels)
    inputs = features[0].reshape(pixels, channels).astype(jnp.float32)
    normed_one, inverse_one, pre_one = norm_forward(inputs, norm_gains[0], norm_shifts[0], members)
    act_one = swish(pre_one).astype(jnp.bfloat16).reshape(grid_shape)
    middle, taps_one = conv_forward(act_one, row_mask, conv_weights[0], conv_biases[0])
    normed_two, inverse_two, pre_two = norm_forward(middle, norm_gains[1], norm_shifts[1], members)
    act_two = swish(pre_two).astype(jnp.bfloat16).reshape(grid_shape)
    branch, taps_two = conv_forward(act_two, row_mask, conv_weights[1], conv_biases[1])
    residual = inputs + branch
    normed_three, inverse_three, pre_three = norm_forward(
        residual, norm_gains[2], norm_shifts[2], members
    )
    attn_input = pre_three.astype(jnp.bfloat16)
    mixed = jnp.dot(attn_input, qkv_weight, preferred_element_type=jnp.float32)
    queries = (mixed[:, :channels] + qv_bias[0]).astype(jnp.bfloat16)
    key_rows = mixed[:, channels : 2 * channels].astype(jnp.bfloat16)
    value_rows = (mixed[:, 2 * channels :] + qv_bias[1]).astype(jnp.bfloat16)
    running_max = jnp.full((pixels,), masked_score, jnp.float32)
    key_piece = lax.all_gather(key_rows, "height", axis=0, tiled=True)
    value_piece = lax.all_gather(value_rows, "height", axis=0, tiled=True)
    scores = (
        lax.dot_general(
            queries, key_piece, (((1,), (1,)), ((), ())), preferred_element_type=jnp.float32
        )
        * score_scale
    )
    same_tile = query_ids[:, None] == key_ids[None, :]
    scores = jnp.where(same_tile, scores, masked_score)
    new_max = jnp.maximum(running_max, jnp.max(scores, axis=1))
    weights = jnp.where(same_tile, jnp.exp(scores - new_max[:, None]), 0.0)
    summed_out = jnp.dot(
        weights.astype(jnp.bfloat16), value_piece, preferred_element_type=jnp.float32
    )
    total_weight = jnp.sum(weights, axis=1)
    log_total = new_max + jnp.log(total_weight)
    attended = summed_out / total_weight[:, None]
    attended_low = attended.astype(jnp.bfloat16)
    output = (
        residual
        + jnp.dot(attended_low, proj_weight, preferred_element_type=jnp.float32)
        + proj_bias
    )
    out_grad = cotangent[0].reshape(pixels, channels)
    out_grad_full = out_grad.astype(jnp.float32)
    proj_grad = lax.dot_general(
        attended_low, out_grad, (((0,), (0,)), ((), ())), preferred_element_type=jnp.float32
    )
    proj_bias_grad = jnp.sum(out_grad_full, axis=0)
    attended_grad = lax.dot_general(
        out_grad, proj_weight, (((1,), (1,)), ((), ())), preferred_element_type=jnp.float32
    ).astype(jnp.bfloat16)
    row_dots = jnp.sum(attended_grad.astype(jnp.float32) * attended, axis=1)
    block_rows = pixels * min(height_size, 8)
    zero_block = jnp.zeros((pixels, channels), jnp.float32)
    key_all, value_all = (
        lax.all_gather(key_rows, "height", axis=0, tiled=True),
        lax.all_gather(value_rows, "height", axis=0, tiled=True),
    )
    query_all, grad_all = (
        lax.all_gather(queries, "height", axis=0, tiled=True),
        lax.all_gather(attended_grad, "height", axis=0, tiled=True),
    )
    total_all, dots_all = (
        lax.all_gather(log_total, "height", axis=0, tiled=True),
        lax.all_gather(row_dots, "height", axis=0, tiled=True),
    )

    def own_query_step(running, block_index):
        offset = block_index * block_rows
        key_part = take_rows(key_all, offset, block_rows)
        rounded, score_grad = score_grads(
            queries,
            attended_grad,
            log_total,
            row_dots,
            query_ids,
            key_part,
            take_rows(value_all, offset, block_rows),
            take_rows(key_ids, offset, block_rows),
            score_scale,
        )
        return (
            running
            + jnp.dot(score_grad, key_part, preferred_element_type=jnp.float32) * score_scale,
            None,
        )

    def own_key_step(running, block_index):
        offset = block_index * block_rows
        query_part = take_rows(query_all, offset, block_rows)
        grad_part = take_rows(grad_all, offset, block_rows)
        rounded, score_grad = score_grads(
            query_part,
            grad_part,
            take_rows(total_all, offset, block_rows),
            take_rows(dots_all, offset, block_rows),
            take_rows(key_ids, offset, block_rows),
            key_rows,
            value_rows,
            query_ids,
            score_scale,
        )
        key_part = (
            lax.dot_general(
                score_grad, query_part, (((0,), (0,)), ((), ())), preferred_element_type=jnp.float32
            )
            * score_scale
        )
        value_part = lax.dot_general(
            rounded, grad_part, (((0,), (0,)), ((), ())), preferred_element_type=jnp.float32
        )
        return ((running[0] + key_part, running[1] + value_part), None)

    block_count = key_all.shape[0] // block_rows
    query_grad, unused_one = lax.scan(own_query_step, zero_block, jnp.arange(block_count))
    (key_grad, value_grad), unused_two = lax.scan(
        own_key_step, (zero_block, zero_block), jnp.arange(block_count)
    )
    query_low = query_grad.astype(jnp.bfloat16)
    key_low = key_grad.astype(jnp.bfloat16)
    value_low = value_grad.astype(jnp.bfloat16)
    stacked_grad = jnp.concatenate([query_low, key_low, value_low], axis=1)
    qkv_grad = lax.dot_general(
        attn_input, stacked_grad, (((0,), (0,)), ((), ())), preferred_element_type=jnp.float32
    )
    qv_grad = jnp.stack(
        [
            jnp.sum(query_low.astype(jnp.float32), axis=0),
            jnp.sum(value_low.astype(jnp.float32), axis=0),
        ]
    )
    normed_grad = lax.dot_general(
        stacked_grad, qkv_weight, (((1,), (1,)), ((), ())), preferred_element_type=jnp.float32
    )
    back_three, gain_three, shift_three = norm_backward(
        normed_grad, normed_three, inverse_three, norm_gains[2], members
    )
    residual_grad = out_grad_full + back_three
    grad_two = residual_grad.astype(jnp.bfloat16).reshape(grid_shape)
    act_two_grad, weight_two_grad, bias_two_grad = conv_backward(
        grad_two, row_mask, conv_weights[1], taps_two
    )
    middle_grad, gain_two, shift_two = norm_backward(
        act_two_grad * swish_slope(pre_two), normed_two, inverse_two, norm_gains[1], members
    )
    grad_one = middle_grad.astype(jnp.bfloat16).reshape(grid_shape)
    act_one_grad, weight_one_grad, bias_one_grad = conv_backward(
        grad_one, row_mask, conv_weights[0], taps_one
    )
    input_back, gain_one, shift_one = norm_backward(
        act_one_grad * swish_slope(pre_one), normed_one, inverse_one, norm_gains[0], members
    )
    input_grad = residual_grad + input_back
    conv_grad = jnp.stack([weight_one_grad, weight_two_grad])
    conv_part = lax.psum_scatter(conv_grad, "height", scatter_dimension=4, tiled=True)
    conv_part = lax.psum_scatter(
        conv_part.astype(jnp.bfloat16), "canvas", scatter_dimension=3, tiled=True
    ).astype(jnp.float32)
    summed = lax.psum(
        (
            jnp.stack([gain_one, gain_two, gain_three]),
            jnp.stack([shift_one, shift_two, shift_three]),
            jnp.stack([bias_one_grad, bias_two_grad]),
            qkv_grad,
            qv_grad,
            proj_grad,
            proj_bias_grad,
        ),
        ("canvas", "height"),
    )
    return (
        output.astype(jnp.bfloat16).reshape((1,) + grid_shape),
        input_grad.astype(jnp.bfloat16).reshape((1,) + grid_shape),
        summed[0],
        summed[1],
        conv_part,
        summed[2],
        summed[3],
        summed[4],
        summed[5],
        summed[6],
    )


def fold(block):
    rows, width = block.shape
    return jnp.sum(block.reshape(rows // 8, 8, width), axis=0)


def group_lanes(block, group):
    lane = lax.broadcasted_iota(jnp.int32, block.shape, 1)
    width = block.shape[1]
    step = 1
    while step < group:
        above = pltpu.roll(block, step, 1)
        below = pltpu.roll(block, width - step, 1)
        block = block + jnp.where((lane & step) != 0, above, below)
        step *= 2
    return block


def group_mean(partial, members):
    spread = group_lanes(partial, partial.shape[1] // GROUPS)
    return jnp.sum(spread, axis=0, keepdims=True) * (1.0 / members)


def widen(block, width):
    return jnp.concatenate([block] * (width // block.shape[1]), axis=1)


def each_block(pixels, block, body, carry=0):
    def step(index, carry):
        return body(pl.ds(pl.multiple_of(index * block, block), block), carry)

    return lax.fori_loop(0, pixels // block, step, carry)


def each_chunk(pixels, body, carry):
    return each_block(pixels, CHUNK, body, carry)


def aligned(start, step):
    return start if isinstance(start, int) else pl.multiple_of(start, step)


class RunningStats:
    def __init__(self, channels):
        self.width = channels // GROUPS
        self.reference = None
        self.sums = self.squares = jnp.zeros((8, channels), jnp.float32)

    def add(self, block):
        if self.reference is None:
            self.reference = group_mean(block[0:8], 8.0 * self.width)
        offset = block - self.reference
        self.sums = self.sums + fold(offset)
        self.squares = self.squares + fold(offset * offset)

    def finish(self, pixels):
        both = group_lanes(jnp.concatenate([self.sums, self.squares], axis=0), self.width)
        share = 1.0 / (pixels * self.width)
        offset = column_total(both[0:8]) * share
        variance = column_total(both[8:16]) * share - offset * offset
        return self.reference + offset, lax.rsqrt(jnp.maximum(variance, 0.0) + epsilon)


def put_taps(taps_ref, block, rows, cols):
    count, channels = block.shape
    place = lax.broadcasted_iota(jnp.int32, block.shape, 0) & (cols - 1)
    left = jnp.where(place == 0, 0.0, pltpu.roll(block, 1, 0))
    right = jnp.where(place == cols - 1, 0.0, pltpu.roll(block, count - 1, 0))
    inner = pl.ds(aligned(rows.start + cols, cols), count)
    taps_ref[inner, 0:channels] = left.astype(jnp.bfloat16)
    taps_ref[inner, channels : 2 * channels] = block.astype(jnp.bfloat16)
    taps_ref[inner, 2 * channels :] = right.astype(jnp.bfloat16)


def clear_edges(taps_ref, cols):
    edge = jnp.zeros((cols, taps_ref.shape[1]), taps_ref.dtype)
    taps_ref[0:cols, :] = edge
    taps_ref[taps_ref.shape[0] - cols :, :] = edge


def begin_conv(taps_ref, product, total_ref, fill, first, cols):
    for start in range(0, total_ref.shape[0], FILL_ROWS):
        for inner in range(start, start + FILL_ROWS, CHUNK):
            fill(pl.ds(inner, CHUNK))
        rows = pl.ds(start, FILL_ROWS)
        total_ref[rows, :] = first(rows, product(taps_ref, pl.ds(start + cols, FILL_ROWS), 1))


def add_rows(taps_ref, product, mask_ref, total_ref, stop, cols):
    rows = pl.ds(0, stop)
    part = product(taps_ref, rows, 0)
    total_ref[rows, :] += widen(mask_ref[0, rows, :], total_ref.shape[1]) * part


def end_conv(taps_ref, product, mask_ref, total_ref, last, cols, old_ref=None, pending=None):
    pixels, channels = total_ref.shape
    old_ref = total_ref if old_ref is None else old_ref
    pending = pixels if pending is None else pending
    for start in range(0, pixels, FILL_ROWS):
        rows = pl.ds(start, FILL_ROWS)
        value = old_ref[rows, :]
        for row_tap in (0, 2) if start >= pending else (2,):
            part = product(taps_ref, pl.ds(start + row_tap * cols, FILL_ROWS), row_tap)
            value = value + widen(mask_ref[row_tap // 2, rows, :], channels) * part
        total_ref[rows, :] = last(rows, value)


def run_conv(taps_ref, product, mask_ref, total_ref, fill, first, last, cols):
    begin_conv(taps_ref, product, total_ref, fill, first, cols)
    add_rows(taps_ref, product, mask_ref, total_ref, total_ref.shape[0], cols)
    end_conv(taps_ref, product, mask_ref, total_ref, last, cols)


def product_forward(weight_ref):
    channels = weight_ref.shape[-1]

    def product(taps_ref, shifted, row_tap):
        return jnp.dot(
            taps_ref[shifted, :],
            weight_ref[row_tap].reshape(3 * channels, channels),
            preferred_element_type=jnp.float32,
        )

    return product


def product_backward(weight_ref):
    def product(taps_ref, shifted, row_tap):
        return lax.dot_general(
            taps_ref[shifted, :],
            weight_ref[row_tap],
            (((1,), (1,)), ((), ())),
            preferred_element_type=jnp.float32,
        )

    return product


def activation(read, mean, inverse, gain, shift, act_ref, taps_ref, cols):
    scale, offset = 0.5 * inverse * gain, 0.5 * shift

    def fill(rows):
        half = (read(rows) - mean) * scale + offset
        act = half * (1.0 + jnp.tanh(half))
        act_ref[rows, :] = act.astype(jnp.bfloat16)
        put_taps(taps_ref, act, rows, cols)

    return fill


def back_means(sums, gain, pixels):
    channels = gain.shape[1]
    members = float(pixels * (channels // GROUPS))
    return group_mean(sums[0] * gain, members), group_mean(sums[1] * gain, members)


def column_total(partial):
    return jnp.sum(partial, axis=0, keepdims=True)


def weight_part(act_ref, narrow, lanes_ref, flip_ref, columns_ref, part_ref, cols):
    pixels, channels = act_ref.shape
    height = lax.axis_index("height")
    share = NARROW // 2
    flip_ref[...] = narrow.T
    own = pl.ds(pl.multiple_of((height % 2) * share, share), share)
    grad = flip_ref[own, :].astype(jnp.float32)
    column = lax.broadcasted_iota(jnp.int32, grad.shape, 1) & (cols - 1)
    for col_tap in range(3):
        shifted = grad
        if col_tap == 0:
            shifted = jnp.where(column == cols - 1, 0.0, pltpu.roll(grad, pixels - 1, 1))
        elif col_tap == 2:
            shifted = jnp.where(column == 0, 0.0, pltpu.roll(grad, 1, 1))
        for row_tap in range(3):
            tap = 3 * row_tap + col_tap
            place = slice(tap * share, (tap + 1) * share)
            if row_tap == 1:
                columns_ref[place, :] = shifted.astype(jnp.bfloat16)
                continue
            side, turn = (0, pixels - cols) if row_tap == 0 else (1, cols)
            masked = (shifted * lanes_ref[side : side + 1, :]).astype(jnp.bfloat16)
            columns_ref[place, :] = pltpu.roll(masked, turn, 1)
    part_ref[...] = jnp.dot(
        columns_ref[...], act_ref[...], preferred_element_type=jnp.float32
    ).astype(jnp.bfloat16)


def begin_back(read, weights_ref, mask_ref, taps_ref, total_ref, stop, cols):
    clear_edges(taps_ref, cols)

    def fill(rows):
        put_taps(taps_ref, read(rows), rows, cols)

    product = product_backward(weights_ref)
    begin_conv(taps_ref, product, total_ref, fill, lambda rows, part: part, cols)
    if stop:
        add_rows(taps_ref, product, mask_ref, total_ref, stop, cols)


def finish_back(
    weights_ref,
    mask_ref,
    taps_ref,
    total_ref,
    read,
    table_ref,
    which,
    cols,
    old_ref=None,
    pending=None,
):
    mean, inverse, gain, shift = norm_rows(table_ref, which)
    scale, offset = 0.5 * inverse * gain, 0.5 * shift
    sums = []

    def slope(rows, value):
        centered = read(rows) - mean
        half = centered * scale + offset
        turn = jnp.tanh(half)
        double = value * ((1.0 + turn) * (1.0 + half * (1.0 - turn)))
        sums.append((fold(double), fold(double * centered)))
        return double

    product = product_backward(weights_ref)
    end_conv(taps_ref, product, mask_ref, total_ref, slope, cols, old_ref, pending)
    plain, cross = sum(pair[0] for pair in sums), sum(pair[1] for pair in sums)
    return 0.5 * plain, 0.5 * inverse * cross


def norm_back(total_ref, double, sums, read, table_ref, which, pixels, scales_ref=None):
    mean, inverse, gain, shift = norm_rows(table_ref, which)
    mean_grad, mean_cross = back_means(sums, gain, pixels)
    slope = inverse * gain * (0.5 if double else 1.0)
    level, tilt = inverse * mean_grad, inverse * inverse * mean_cross
    if scales_ref is not None:
        for row, scales in enumerate((mean, slope, level, tilt)):
            scales_ref[row : row + 1, :] = scales

    def back(rows, inner):
        return total_ref[inner, :] * slope - level - (read(rows) - mean) * tilt

    return back


def own_lanes():
    block = lax.axis_index("height") // 2
    return pl.ds(pl.multiple_of(block * NARROW, NARROW), NARROW)


def narrow_back(total_ref, value_ref, scales_ref):
    lanes = own_lanes()
    mean, slope, level, tilt = (scales_ref[row : row + 1, lanes] for row in range(4))
    return total_ref[:, lanes] * slope - level - (value_ref[:, lanes] - mean) * tilt


def scaled_back(total_ref, value_ref, scales_ref, rows, inner):
    mean, slope, level, tilt = (scales_ref[row : row + 1, :] for row in range(4))
    return total_ref[inner, :] * slope - level - (value_ref[rows, :].astype(jnp.float32) - mean) * tilt


def turn_kernel(
    grad_ref,
    total_three_ref,
    scales_ref,
    residual_ref,
    mask_ref,
    weights_ref,
    old_sums_ref,
    total_ref,
    taps_ref,
    sums_ref,
    *,
    cols,
):
    grad_sums = []

    def read(rows):
        grad = scaled_back(total_three_ref, residual_ref, scales_ref, rows, rows)
        grad = grad_ref[rows, :].astype(jnp.float32) + grad
        grad = grad.astype(jnp.bfloat16).astype(jnp.float32)
        grad_sums.append(fold(grad))
        return grad

    begin_back(read, weights_ref.at[1], mask_ref, taps_ref, total_ref, EARLY_ROWS, cols)
    sums_ref[...] = old_sums_ref[...]
    sums_ref[7:8, :] = column_total(sum(grad_sums))


def norm_rows(table_ref, which):
    picks = (2 * which, 2 * which + 1, 6 + which, 9 + which)
    return tuple(table_ref[pick : pick + 1, :] for pick in picks)


def build_masks(ids_ref, mask_ref, lanes_ref, id_rows_ref, id_cols_ref, cols):
    rows = ids_ref.shape[1]

    def one_row(row, carry):
        here = ids_ref[0, row]
        place = pl.ds(pl.multiple_of(row * cols, cols), cols)
        id_rows_ref[place, :] = jnp.full((cols, LANES), here, jnp.int32)
        for side, other in ((0, row - 1), (1, row + 1)):
            inside = jnp.logical_and(other >= 0, other < rows)
            other_id = ids_ref[0, jnp.clip(other, 0, rows - 1)]
            same = jnp.where(jnp.logical_and(inside, other_id == here), 1.0, 0.0)
            mask_ref[side, place, :] = jnp.full((cols, LANES), same, jnp.float32)
        return carry

    lax.fori_loop(0, rows, one_row, 0)
    lane = lax.broadcasted_iota(jnp.int32, (8, LANES), 1)
    each = LANES // cols
    for block in range(rows // each):
        ids = jnp.full((8, LANES), ids_ref[0, block * each], jnp.int32)
        for step in range(1, each):
            ids = jnp.where(lane >= step * cols, ids_ref[0, block * each + step], ids)
        id_cols_ref[:, block * LANES : (block + 1) * LANES] = ids
    ids = id_cols_ref[...].astype(jnp.float32)
    pixels = ids.shape[1]
    pixel = lax.broadcasted_iota(jnp.int32, ids.shape, 1)
    above = jnp.where(pixel < cols, -1.0, pltpu.roll(ids, cols, 1))
    below = jnp.where(pixel >= pixels - cols, -1.0, pltpu.roll(ids, pixels - cols, 1))
    lanes_ref[0:1, :] = jnp.where(above == ids, 1.0, 0.0)[0:1]
    lanes_ref[1:2, :] = jnp.where(below == ids, 1.0, 0.0)[0:1]


def hold_kernel(
    ids_hbm,
    gains_hbm,
    shifts_hbm,
    biases_hbm,
    weights_hbm,
    qkv_hbm,
    proj_hbm,
    qv_bias_hbm,
    proj_bias_hbm,
    weights_ref,
    turned_ref,
    qkv_ref,
    proj_ref,
    table_ref,
    mask_ref,
    lanes_ref,
    id_rows_ref,
    id_cols_ref,
    ids_ref,
    gains_ref,
    shifts_ref,
    biases_ref,
    qv_bias_ref,
    proj_bias_ref,
    sems,
    *,
    cols,
):
    channels = weights_ref.shape[-1]
    small = [
        (ids_hbm, ids_ref),
        (gains_hbm, gains_ref),
        (shifts_hbm, shifts_ref),
        (biases_hbm, biases_ref),
        (qv_bias_hbm, qv_bias_ref),
        (proj_bias_hbm, proj_bias_ref),
    ]
    large = [(weights_hbm, weights_ref), (qkv_hbm, qkv_ref), (proj_hbm, proj_ref)]
    for which in range(2):
        for row_tap in range(3):
            for col_tap in range(3):
                place = slice(col_tap * channels, (col_tap + 1) * channels)
                large.append(
                    (
                        weights_hbm.at[which, 2 - row_tap, 2 - col_tap],
                        turned_ref.at[which, row_tap, :, place],
                    )
                )
    copies = [
        pltpu.make_async_copy(source, target, sems.at[index])
        for index, (source, target) in enumerate(small + large)
    ]
    for copy in copies:
        copy.start()
    for copy in copies[: len(small)]:
        copy.wait()
    build_masks(ids_ref, mask_ref, lanes_ref, id_rows_ref, id_cols_ref, cols)
    table_ref[6:9, :] = gains_ref[...]
    table_ref[9:12, :] = shifts_ref[...]
    table_ref[12:14, :] = biases_ref[...]
    table_ref[14:16, :] = qv_bias_ref[...]
    table_ref[16:17, :] = proj_bias_ref[...]
    for copy in copies[len(small) :]:
        copy.wait()


def conv_kernel(*refs, cols, count):
    pieces, refs = refs[:count], refs[count:]
    (
        weights_ref,
        params_ref,
        mask_ref,
        features_ref,
        act_one_ref,
        middle_ref,
        act_two_ref,
        residual_ref,
        table_ref,
        own_ref,
        taps_ref,
        sem,
    ) = refs
    pixels, channels = features_ref.shape
    wide = jnp.float32
    own_copy = pltpu.make_async_copy(pieces[0], own_ref, sem)
    own_copy.start()
    table_ref[...] = params_ref[...]
    clear_edges(taps_ref, cols)

    def read_input(rows):
        return features_ref[rows, :].astype(wide)

    def read_middle(rows):
        return middle_ref[rows, :]

    height = lax.axis_index("height")
    own_pixels = pixels // count
    seen = RunningStats(channels)
    for place in list(range(1, count)) + [0]:
        if place == 0:
            own_copy.wait()
        piece = (pieces[place] if place else own_ref)[0:own_pixels, :]
        start = pl.multiple_of((height ^ place) * own_pixels, own_pixels)
        features_ref[pl.ds(start, own_pixels), :] = piece
        seen.add(piece.astype(wide))
    table_ref[0:1, :], table_ref[1:2, :] = seen.finish(pixels)
    seen = RunningStats(channels)

    def keep(rows, value):
        seen.add(value)
        return value

    run_conv(
        taps_ref,
        product_forward(weights_ref.at[0]),
        mask_ref,
        middle_ref,
        activation(read_input, *norm_rows(table_ref, 0), act_one_ref, taps_ref, cols),
        lambda rows, part: part + table_ref[12:13, :],
        keep,
        cols,
    )
    table_ref[2:3, :], table_ref[3:4, :] = seen.finish(pixels)
    seen = RunningStats(channels)
    run_conv(
        taps_ref,
        product_forward(weights_ref.at[1]),
        mask_ref,
        residual_ref,
        activation(read_middle, *norm_rows(table_ref, 1), act_two_ref, taps_ref, cols),
        lambda rows, part: part + (read_input(rows) + table_ref[13:14, :]),
        keep,
        cols,
    )
    table_ref[4:5, :], table_ref[5:6, :] = seen.finish(pixels)


def score_kernel(
    qkv_ref,
    proj_ref,
    residual_ref,
    table_ref,
    id_rows_ref,
    id_cols_ref,
    flip_ref,
    query_ref,
    key_flip_ref,
    value_ref,
    soft_ref,
    out_flip_ref,
    output_ref,
    normed_ref,
    key_ref,
    value_flip_ref,
    *scores_refs,
    score_scale,
):
    pixels, channels = residual_ref.shape
    own_pixels = output_ref.shape[0]
    wide = jnp.float32
    exponent = score_scale * 1.4426950408889634
    mean, inverse, gain, shift = norm_rows(table_ref, 2)
    scale = inverse * gain

    def normalise(start):
        rows = slice(start, start + KEY_ROWS)
        normed = (residual_ref[rows, :] - mean) * scale + shift
        normed_ref[rows, :] = normed.astype(jnp.bfloat16)

    def project(start):
        rows = slice(start, start + KEY_ROWS)
        normed = normed_ref[rows, :]
        query_ref[rows, :] = (
            jnp.dot(normed, qkv_ref[:, 0:channels], preferred_element_type=wide)
            + table_ref[14:15, :]
        ).astype(jnp.bfloat16)
        keys = jnp.dot(
            normed, qkv_ref[:, channels : 2 * channels], preferred_element_type=wide
        ).astype(jnp.bfloat16)
        key_ref[rows, :] = keys
        key_flip_ref[:, rows] = keys.T
        values = (
            jnp.dot(normed, qkv_ref[:, 2 * channels :], preferred_element_type=wide)
            + table_ref[15:16, :]
        ).astype(jnp.bfloat16)
        value_ref[rows, :] = values
        value_flip_ref[:, rows] = values.T

    normalise(0)
    for start in range(0, pixels, KEY_ROWS):
        if start + KEY_ROWS < pixels:
            normalise(start + KEY_ROWS)
        project(start)
    quarter = flip_ref.shape[0]
    lanes = pl.ds(pl.multiple_of(own_quarter() * quarter, quarter), quarter)
    flip_ref[...] = normed_ref[:, lanes].T
    block = scores_refs[0].shape[1]
    steps = range(0, pixels, KEY_ROWS)

    def score(index):
        rows = slice(index * block, (index + 1) * block)
        for start in steps:
            keys = slice(start, start + KEY_ROWS)
            scores = lax.dot_general(
                key_ref[keys, :],
                query_ref[rows, :],
                (((1,), (1,)), ((), ())),
                preferred_element_type=wide,
            )
            same = widen(id_rows_ref[keys, :], block) == id_cols_ref[0:1, rows]
            scores_refs[index][keys, :] = jnp.where(same, scores, masked_score)

    def soften(index):
        rows = slice(index * block, (index + 1) * block)
        scores_ref = scores_refs[index]
        peak = jnp.full((8, block), masked_score, wide)
        for start in steps:
            scores = scores_ref[start : start + KEY_ROWS, :]
            peak = jnp.maximum(peak, jnp.max(scores.reshape(-1, 8, block), axis=0))
        peak = jnp.max(peak, axis=0, keepdims=True)
        total = jnp.zeros((8, block), wide)
        for start in steps:
            keys = slice(start, start + KEY_ROWS)
            powers = jnp.exp2((scores_ref[keys, :] - peak) * exponent)
            scores_ref[keys, :] = powers
            total = total + fold(powers)
        share = 1.0 / column_total(total)
        for start in steps:
            keys = slice(start, start + KEY_ROWS)
            soft_ref[keys, rows] = (scores_ref[keys, :] * share).astype(jnp.bfloat16)

    score(0)
    for index in range(len(scores_refs)):
        if index + 1 < len(scores_refs):
            score(index + 1)
        soften(index)
        rows = slice(index * block, (index + 1) * block)
        out_flip_ref[:, rows] = jnp.dot(
            value_flip_ref[...], soft_ref[:, rows], preferred_element_type=wide
        ).astype(jnp.bfloat16)
    height = lax.axis_index("height")
    own = pl.ds(pl.multiple_of(height * own_pixels, own_pixels), own_pixels)
    output_ref[...] = (
        residual_ref[own, :]
        + lax.dot_general(
            out_flip_ref[:, own],
            proj_ref[...],
            (((0,), (0,)), ((), ())),
            preferred_element_type=wide,
        )
        + table_ref[16:17, :]
    ).astype(jnp.bfloat16)


def own_quarter():
    height = lax.axis_index("height")
    return (height & 1) * 2 + ((height >> 1) & 1)


def attention_kernel(
    proj_ref,
    flip_ref,
    query_ref,
    key_flip_ref,
    value_ref,
    soft_ref,
    out_flip_ref,
    *refs,
    score_scale,
    count,
):
    pieces, (grad_ref, packed_ref, sums_ref), refs = (
        refs[:count],
        refs[count : count + 3],
        refs[count + 3 :],
    )
    pixels, channels = query_ref.shape
    blocks = pixels // SCORE_ROWS
    grads_refs, refs = refs[-blocks:], refs[:-blocks]
    *mixed_refs, mixed_ref, back_ref, score_grad_ref = refs
    wide = jnp.float32
    height = lax.axis_index("height")
    own_pixels = pixels // count
    for place, piece in enumerate(pieces):
        start = pl.multiple_of((height ^ place) * own_pixels, own_pixels)
        last = piece.shape[0]
        grad_ref[pl.ds(start, own_pixels), :] = piece[last - own_pixels : last, :]
    quarter = channels // 4
    own = pl.ds(pl.multiple_of(own_quarter() * quarter, quarter), quarter)
    block, count = SCORE_ROWS, blocks
    steps = range(0, pixels, KEY_ROWS)

    def block_rows(index):
        return slice(index * block, (index + 1) * block)

    for start in range(0, pixels, 2 * block):
        rows = slice(start, start + 2 * block)
        back_ref[rows, :] = lax.dot_general(
            grad_ref[rows, :],
            proj_ref[...],
            (((1,), (1,)), ((), ())),
            preferred_element_type=wide,
        ).astype(jnp.bfloat16)

    def weigh(index):
        total = jnp.zeros((8, block), wide)
        for start in steps:
            keys = slice(start, start + KEY_ROWS)
            weight_grad = lax.dot_general(
                value_ref[keys, :],
                back_ref[block_rows(index), :],
                (((1,), (1,)), ((), ())),
                preferred_element_type=wide,
            )
            grads_refs[index][keys, :] = weight_grad
            total = total + fold(soft_ref[keys, block_rows(index)].astype(wide) * weight_grad)
        return column_total(total)

    def slope(index, dots):
        for start in steps:
            keys = slice(start, start + KEY_ROWS)
            weights = soft_ref[keys, block_rows(index)].astype(wide)
            score_grad_ref[keys, block_rows(index)] = (
                weights * (grads_refs[index][keys, :] - dots)
            ).astype(jnp.bfloat16)

    dots = weigh(0)
    for index in range(count):
        now, rows = dots, block_rows(index)
        if index + 1 < count:
            dots = weigh(index + 1)
        slope(index, now)
        packed_ref[rows, 2 * channels :] = jnp.dot(
            soft_ref[rows, :], back_ref[...], preferred_element_type=wide
        ).astype(jnp.bfloat16)
        query_grad = jnp.dot(
            key_flip_ref[...], score_grad_ref[:, rows], preferred_element_type=wide
        )
        packed_ref[rows, 0:channels] = (query_grad * score_scale).astype(jnp.bfloat16).T
    for start in range(0, pixels, 2 * block):
        rows = slice(start, start + 2 * block)
        packed_ref[rows, channels : 2 * channels] = (
            jnp.dot(score_grad_ref[rows, :], query_ref[...], preferred_element_type=wide)
            * score_scale
        ).astype(jnp.bfloat16)

    def pack(rows, carry):
        return (
            carry[0] + fold(packed_ref[rows, 0:channels].astype(wide)),
            carry[1] + fold(packed_ref[rows, 2 * channels :].astype(wide)),
            carry[2] + fold(grad_ref[rows, :].astype(wide)),
        )

    zeros = jnp.zeros((8, channels), wide)
    totals = zeros, zeros, zeros
    for start in range(0, pixels, CHUNK):
        totals = pack(pl.ds(start, CHUNK), totals)
    sums_ref[...] = jnp.zeros(sums_ref.shape, wide)
    for row, total in enumerate(totals):
        sums_ref[8 + row : 9 + row, :] = column_total(total)
    mixed_ref[:, 0 : 3 * channels] = jnp.dot(
        flip_ref[...], packed_ref[...], preferred_element_type=wide
    ).astype(jnp.bfloat16)
    mixed_ref[:, 3 * channels :] = jnp.dot(
        out_flip_ref[own, :], grad_ref[...], preferred_element_type=wide
    ).astype(jnp.bfloat16)
    share = quarter // len(mixed_refs)
    me = lax.axis_index("canvas")
    for step, target in enumerate(mixed_refs):
        target[...] = mixed_ref[pl.ds(pl.multiple_of((me ^ step) * share, share), share), :]


def third_kernel(
    qkv_ref,
    grad_ref,
    packed_ref,
    residual_ref,
    table_ref,
    act_two_ref,
    lanes_ref,
    old_sums_ref,
    total_ref,
    scales_ref,
    sums_ref,
    part_ref,
    flip_ref,
    columns_ref,
    *,
    cols,
):
    pixels, channels = residual_ref.shape
    block = 2 * FILL_ROWS
    wide = jnp.float32
    mean, inverse, gain, shift = norm_rows(table_ref, 2)
    zeros = jnp.zeros((8, channels), wide)

    sums = (zeros, zeros)
    for start in range(0, pixels, block):
        rows = pl.ds(start, block)
        normed_grad = lax.dot_general(
            packed_ref[rows, :], qkv_ref[...], (((1,), (1,)), ((), ())), preferred_element_type=wide
        )
        total_ref[rows, :] = normed_grad
        centered = residual_ref[rows, :] - mean
        sums = sums[0] + fold(normed_grad), sums[1] + fold(normed_grad * centered)
    sums = sums[0], sums[1] * inverse
    sums_ref[...] = old_sums_ref[...]
    sums_ref[5:6, :] = column_total(sums[1])
    sums_ref[6:7, :] = column_total(sums[0])
    norm_back(
        total_ref, False, sums, lambda rows: residual_ref[rows, :], table_ref, 2, pixels, scales_ref
    )
    narrow = narrow_back(total_ref, residual_ref, scales_ref)
    narrow = (grad_ref[:, own_lanes()].astype(wide) + narrow).astype(jnp.bfloat16)
    weight_part(act_two_ref, narrow, lanes_ref, flip_ref, columns_ref, part_ref, cols)


def second_kernel(
    old_total_ref,
    taps_ref,
    middle_ref,
    table_ref,
    act_one_ref,
    mask_ref,
    lanes_ref,
    weights_ref,
    old_sums_ref,
    part_two_ref,
    total_ref,
    scales_ref,
    sums_ref,
    keep_one_ref,
    send_one_ref,
    keep_two_ref,
    send_two_ref,
    flip_ref,
    columns_ref,
    part_ref,
    *,
    cols,
):
    pixels, channels = middle_ref.shape

    def read(rows):
        return middle_ref[rows, :]

    sums = finish_back(
        weights_ref.at[1],
        mask_ref,
        taps_ref,
        total_ref,
        read,
        table_ref,
        1,
        cols,
        old_total_ref,
        EARLY_ROWS,
    )
    norm_back(total_ref, True, sums, read, table_ref, 1, pixels, scales_ref)
    narrow = narrow_back(total_ref, middle_ref, scales_ref).astype(jnp.bfloat16)
    weight_part(act_one_ref, narrow, lanes_ref, flip_ref, columns_ref, part_ref, cols)
    sums_ref[...] = old_sums_ref[...]
    sums_ref[2:3, :] = column_total(sums[1])
    sums_ref[3:4, :] = column_total(sums[0])
    keep_half(part_ref, keep_one_ref, send_one_ref)
    keep_half(part_two_ref, keep_two_ref, send_two_ref)


def near_far():
    core = lax.axis_index("height") & 1
    return 1 + core, 2 - core


def keep_half(source_ref, keep_ref, send_ref):
    me = lax.axis_index("canvas")
    near, far = near_far()
    rows, width = keep_ref.shape[0] // 2, keep_ref.shape[1]
    for target_ref, flip in ((keep_ref, 0), (send_ref, near)):
        for slot, other in enumerate((0, far)):
            place = pl.ds(pl.multiple_of((me ^ flip ^ other) * width, width), width)
            target_ref[slot * rows : (slot + 1) * rows, :] = source_ref[:, place]


def first_kernel(
    total_two_ref,
    scales_ref,
    middle_ref,
    features_ref,
    table_ref,
    mask_ref,
    old_sums_ref,
    weights_ref,
    own_ref,
    sums_ref,
    partial_ref,
    total_ref,
    taps_ref,
    *,
    cols,
):
    def read(rows):
        return features_ref[rows, :].astype(jnp.float32)

    grad_sums = []

    def read_grad(rows):
        grad = scaled_back(total_two_ref, middle_ref, scales_ref, rows, rows)
        grad = grad.astype(jnp.bfloat16).astype(jnp.float32)
        grad_sums.append(fold(grad))
        return grad

    weights = weights_ref.at[0]
    begin_back(read_grad, weights, mask_ref, taps_ref, total_ref, total_ref.shape[0], cols)
    sums = finish_back(weights, mask_ref, taps_ref, total_ref, read, table_ref, 0, cols)
    partial_ref[0:8, :], partial_ref[8:16, :] = sums
    sums_ref[...] = old_sums_ref[...]
    sums_ref[0:1, :] = column_total(sums[1])
    sums_ref[1:2, :] = column_total(sums[0])
    sums_ref[4:5, :] = column_total(sum(grad_sums))
    count = own_ref.shape[0]
    own = pl.ds(pl.multiple_of(lax.axis_index("height") * count, count), count)
    own_ref[...] = total_ref[own, :]


def own_kernel(
    own_ref,
    partial_ref,
    features_ref,
    grad_ref,
    total_three_ref,
    residual_ref,
    scales_ref,
    table_ref,
    input_grad_ref,
):
    def read(rows):
        return features_ref[rows, :].astype(jnp.float32)

    sums = partial_ref[0:8, :], partial_ref[8:16, :]
    pixels = features_ref.shape[0]
    back = norm_back(own_ref, True, sums, read, table_ref, 0, pixels)
    count = own_ref.shape[0]
    own = pl.ds(pl.multiple_of(lax.axis_index("height") * count, count), count)
    total = scaled_back(total_three_ref, residual_ref, scales_ref, own, own)
    total = grad_ref[own, :].astype(jnp.float32) + total
    input_grad_ref[...] = (total + back(own, slice(0, count))).astype(jnp.bfloat16)


def place_kernel(*refs):
    joints, packed_ref = refs[:-1], refs[-1]
    share = packed_ref.shape[0] // len(joints)
    me = lax.axis_index("canvas")
    for step, joint in enumerate(joints):
        place = pl.ds(pl.multiple_of((me ^ step) * share, share), share)
        packed_ref[place, :] = joint[...]


def cut_kernel(packed_ref, *half_refs):
    rows = half_refs[0].shape[0]
    for index, half_ref in enumerate(half_refs):
        half_ref[...] = packed_ref[index * rows : (index + 1) * rows, :]


def spread_quarters(packed, flips, qkv_ref, proj_ref, qkv_hbm, proj_hbm, sems):
    quarter = packed[0].shape[0]
    inner = qkv_ref.shape[2]
    copies = []
    for index, packed_ref in enumerate(packed):
        owner = own_quarter() ^ flips[index]
        rows = pl.ds(pl.multiple_of(owner * quarter, quarter), quarter)
        qkv_ref[index] = packed_ref[:, 0:inner].astype(jnp.float32)
        proj_ref[index] = packed_ref[:, inner:].astype(jnp.float32)
        for which, (held, target) in enumerate(((qkv_ref, qkv_hbm), (proj_ref, proj_hbm))):
            copy = pltpu.make_async_copy(held.at[index], target.at[rows, :], sems.at[index, which])
            copy.start()
            copies.append(copy)
    return copies


def join_kernel(*refs):
    packed, (qkv_hbm, proj_hbm, qkv_ref, proj_ref, sems) = refs[:-5], refs[-5:]
    copies = spread_quarters(packed, [0, 2], qkv_ref, proj_ref, qkv_hbm, proj_hbm, sems)
    for copy in copies:
        copy.wait()


def halve_kernel(keep_ref, got_ref, hold_ref, send_ref):
    total = keep_ref[...].astype(jnp.float32) + got_ref[...].astype(jnp.float32)
    rows = hold_ref.shape[0]
    hold_ref[...] = total[0:rows]
    send_ref[0:rows, :] = total[rows:].astype(jnp.bfloat16)


def halve_both_kernel(
    keep_ref, got_ref, keep_two_ref, got_two_ref, hold_ref, send_ref, hold_two_ref
):
    rows = hold_ref.shape[0]
    halve_kernel(keep_ref, got_ref, hold_ref, send_ref)
    halve_kernel(keep_two_ref, got_two_ref, hold_two_ref, send_ref.at[rows : 2 * rows, :])


def last_kernel(
    chip_ref,
    both_a_ref,
    both_b_ref,
    old_qkv,
    old_proj,
    qkv_hbm,
    proj_hbm,
    qkv_ref,
    proj_ref,
    sems,
):
    copies = []
    rows = both_a_ref.shape[0]
    inner = qkv_ref.shape[2]
    chips = (chip_ref.at[0:rows, :], chip_ref.at[rows : 2 * rows, :])
    for index, piece_ref in enumerate((*chips, both_a_ref, both_b_ref)):
        start = ((own_quarter() ^ (1 if index < 2 else 3)) * 2 + index % 2) * rows
        target = pl.ds(pl.multiple_of(start, rows), rows)
        qkv_ref[index] = piece_ref[:, 0:inner].astype(jnp.float32)
        proj_ref[index] = piece_ref[:, inner:].astype(jnp.float32)
        for which, (held, whole) in enumerate(((qkv_ref, qkv_hbm), (proj_ref, proj_hbm))):
            copy = pltpu.make_async_copy(held.at[index], whole.at[target, :], sems.at[index, which])
            copy.start()
            copies.append(copy)
    for copy in copies:
        copy.wait()


def sums_kernel(
    sums_ref,
    got_sums_ref,
    hold_one_ref,
    hold_two_ref,
    got_ref,
    share_ref,
    gains_ref,
    shifts_ref,
    conv_ref,
    qv_ref,
    bias_ref,
):
    rows = hold_one_ref.shape[0]
    for which, hold_ref in enumerate((hold_one_ref, hold_two_ref)):
        got = got_ref[which * rows : (which + 1) * rows, :].astype(jnp.float32)
        share_ref[which] = (hold_ref[...] + got).reshape(share_ref.shape[1:])
    total = sums_ref[...] + got_sums_ref[...]
    for row, start in enumerate((0, 2, 5)):
        gains_ref[row : row + 1, :] = total[start : start + 1]
        shifts_ref[row : row + 1, :] = total[start + 1 : start + 2]
    conv_ref[0:1, :] = total[4:5]
    conv_ref[1:2, :] = total[7:8]
    qv_ref[...] = total[8:10]
    bias_ref[...] = total[10:11]


def call_kernel(kernel, outputs, scratch, operands, places, flops, limit, out_places=None, aliases={}):
    out_places = out_places or "v" * len(outputs)
    spaces = {
        "v": pl.BlockSpec(memory_space=pltpu.VMEM),
        "s": pl.BlockSpec(memory_space=pltpu.SMEM),
        "h": pl.BlockSpec(memory_space=pl.ANY),
        "o": pl.BlockSpec(memory_space=pltpu.VMEM),
        "a": pl.BlockSpec(memory_space=pl.ANY),
    }
    moved = 8 * flops // LANES
    held = {"v": pltpu.VMEM, "h": pltpu.HBM, "o": jax.ShapeDtypeStruct}
    operands = [
        pltpu.with_memory_space_constraint(array, pltpu.HBM) if place == "h" else array
        for array, place in zip(operands, places)
    ]
    return pl.pallas_call(
        kernel,
        out_shape=[held[place](*output) for output, place in zip(outputs, out_places)],
        in_specs=[spaces[place] for place in places],
        out_specs=[spaces[place] for place in out_places],
        scratch_shapes=scratch,
        input_output_aliases=aliases,
        compiler_params=pltpu.CompilerParams(vmem_limit_bytes=limit * 2**20),
        cost_estimate=pl.CostEstimate(flops=flops, bytes_accessed=moved, transcendentals=0),
    )(*operands)


def send_height(block, step):
    size = lax.axis_size("height")
    return lax.ppermute(block, "height", [(i, i ^ step) for i in range(size)])


def with_cores(blocks, other):
    pieces = [blocks[0], other]
    for block in blocks[1:]:
        pieces += [block, send_height(block, 1)]
    return pieces


def send_canvas(block, step):
    size = lax.axis_size("canvas")
    return lax.ppermute(block, "canvas", [(i, i ^ step) for i in range(size)])


def send_phase(block, phase):
    canvases, size = lax.axis_size("canvas"), lax.axis_size("height")
    pairs = []
    for canvas in range(canvases):
        for height in range(size):
            step = 2 if (height ^ phase) & 1 else 1
            pairs.append((canvas * size + height, (canvas ^ step) * size + height))
    return lax.ppermute(block, ("canvas", "height"), pairs)


def trade_canvas(pieces):
    return [pieces[0]] + [send_canvas(piece, step) for step, piece in enumerate(pieces) if step]


def whole_canvas(
    features,
    tile_ids,
    norm_gains,
    norm_shifts,
    conv_weights,
    conv_biases,
    qkv_weight,
    qv_bias,
    proj_weight,
    proj_bias,
    cotangent,
):
    height_size = lax.axis_size("height")
    canvas_size = lax.axis_size("canvas")
    local_rows, cols, channels = features.shape[1:]
    all_rows = tile_ids.shape[1]
    pixels = all_rows * cols
    own_pixels = local_rows * cols
    out_share = channels // height_size
    ci_share = channels // canvas_size
    quarter = channels // 4
    row_share = quarter // canvas_size
    low, wide = jnp.bfloat16, jnp.float32

    own_features = features.reshape(own_pixels, channels)
    own_grad = cotangent.reshape(own_pixels, channels)
    steps = range(2, height_size, 2)
    held_features = [own_features] + [send_height(own_features, step) for step in steps]
    plane = ((pixels, channels), low)
    plane_wide = ((pixels, channels), wide)
    sums_shape = ((16, channels), wide)
    mixed_shapes = [((row_share, 4 * channels), low)] * canvas_size
    taps = pltpu.VMEM((pixels + 2 * cols, 3 * channels), low)
    held_wide = pltpu.VMEM((pixels, channels), wide)
    flipped = pltpu.VMEM((channels, pixels), low)
    narrow = pltpu.VMEM((NARROW, pixels), low)
    columns = pltpu.VMEM((9 * out_share, pixels), low)
    part_held = pltpu.VMEM((9 * out_share, channels), low)
    sem = pltpu.SemaphoreType.DMA
    conv_flops = 2 * 9 * pixels * channels * channels
    dot_flops = 2 * pixels * channels * channels
    score_flops = 2 * pixels * pixels * channels
    scale = channels ** (-0.5)

    (
        held_conv,
        turned,
        held_qkv,
        held_proj,
        params,
        mask,
        lane_mask,
        id_rows,
        id_cols,
    ) = call_kernel(
        functools.partial(hold_kernel, cols=cols),
        [
            (conv_weights.shape, low),
            ((2, 3, channels, 3 * channels), low),
            (qkv_weight.shape, low),
            (proj_weight.shape, low),
            ((24, channels), wide),
            ((2, pixels, LANES), wide),
            ((8, pixels), wide),
            ((pixels, LANES), jnp.int32),
            ((8, pixels), jnp.int32),
        ],
        [
            pltpu.SMEM(tile_ids.shape, jnp.int32),
            pltpu.VMEM(norm_gains.shape, wide),
            pltpu.VMEM(norm_shifts.shape, wide),
            pltpu.VMEM(conv_biases.shape, wide),
            pltpu.VMEM(qv_bias.shape, wide),
            pltpu.VMEM((1, channels), wide),
            sem((27,)),
        ],
        [
            tile_ids,
            norm_gains,
            norm_shifts,
            conv_biases,
            conv_weights,
            qkv_weight,
            proj_weight,
            qv_bias,
            proj_bias.reshape(1, channels),
        ],
        "h" * 9,
        conv_flops,
        8,
    )
    held_features[1:] = [
        lax.optimization_barrier((params, block))[1] for block in held_features[1:]
    ]
    other_core = send_height(jnp.concatenate([own_features, own_grad], axis=0), 1)
    pieces = with_cores(held_features, other_core)
    far_grad, *pieces[4::2] = lax.optimization_barrier((own_grad, *held_features[2:]))
    held_grads = [own_grad, send_height(own_grad, 2)]
    held_grads[1], pieces[2] = lax.optimization_barrier((held_grads[1], held_features[1]))
    held_grads += [send_height(far_grad, step) for step in steps[1:]]

    all_features, act_one, middle, act_two, residual, table = call_kernel(
        functools.partial(conv_kernel, cols=cols, count=height_size),
        [plane, plane, plane_wide, plane, plane_wide, ((24, channels), wide)],
        [pltpu.VMEM((own_pixels, channels), low), taps, sem],
        [*pieces, held_conv, params, mask],
        "h" + "v" * (height_size + 2),
        2 * conv_flops,
        16,
    )
    residual, *held_grads = lax.optimization_barrier((residual, *held_grads))
    grad_pieces = with_cores(held_grads, other_core)
    normed_flip, query, key_flip, value, soft, out_flip, output = call_kernel(
        functools.partial(score_kernel, score_scale=scale),
        [
            ((quarter, pixels), low),
            plane,
            ((channels, pixels), low),
            plane,
            ((pixels, pixels), low),
            ((channels, pixels), low),
            ((own_pixels, channels), low),
        ],
        [
            pltpu.VMEM((pixels, channels), low),
            pltpu.VMEM((pixels, channels), low),
            flipped,
            *[pltpu.VMEM((pixels, SCORE_ROWS), wide)] * (pixels // SCORE_ROWS),
        ],
        [
            held_qkv,
            held_proj,
            residual,
            table,
            id_rows,
            id_cols,
        ],
        "vvvvvv",
        3 * dot_flops + 2 * score_flops,
        20,
        "v" * 6 + "o",
    )
    normed_flip, *grad_pieces = lax.optimization_barrier((normed_flip, *grad_pieces))
    all_grad, packed, sums, *mixed = call_kernel(
        functools.partial(attention_kernel, score_scale=scale, count=height_size),
        [plane, ((pixels, 3 * channels), low), sums_shape, *mixed_shapes],
        [
            pltpu.VMEM((quarter, 4 * channels), low),
            pltpu.VMEM((pixels, channels), low),
            pltpu.VMEM((pixels, pixels), low),
            *[pltpu.VMEM((pixels, SCORE_ROWS), wide)] * (pixels // SCORE_ROWS),
        ],
        [held_proj, normed_flip, query, key_flip, value, soft, out_flip, *grad_pieces],
        "v" * (7 + height_size),
        3 * dot_flops + 4 * score_flops,
        20,
    )
    mixed = trade_canvas(mixed)
    total_three, scales_three, sums, part_two = call_kernel(
        functools.partial(third_kernel, cols=cols),
        [plane_wide, ((8, channels), wide), sums_shape, ((9 * out_share, channels), low)],
        [narrow, columns],
        [held_qkv, all_grad, packed, residual, table, act_two, lane_mask, sums],
        "vvvvvvvv",
        3 * dot_flops + conv_flops // height_size,
        16,
    )
    half_total, half_taps, sums = call_kernel(
        functools.partial(turn_kernel, cols=cols),
        [plane_wide, (taps.shape, low), sums_shape],
        [],
        [all_grad, total_three, scales_three, residual, mask, turned, sums],
        "vvvvvvv",
        conv_flops // 2,
        16,
    )
    half_total, *mixed = lax.optimization_barrier((half_total, *mixed))
    mixed_sum = mixed[0].astype(wide)
    for piece in mixed[1:]:
        mixed_sum = mixed_sum + piece.astype(wide)
    mixed_sum = mixed_sum.astype(low)
    joints = trade_canvas([mixed_sum] * canvas_size)
    halves = [((2 * 9 * out_share, ci_share), low)] * 4
    total_two, scales, sums, keep_one, send_one, keep_two, send_two = call_kernel(
        functools.partial(second_kernel, cols=cols),
        [plane_wide, ((8, channels), wide), sums_shape, *halves],
        [narrow, columns, part_held],
        [half_total, half_taps, middle, table, act_one, mask, lane_mask, turned, sums, part_two],
        "v" * 10,
        conv_flops // 2,
        20,
    )
    total_two, *joints = lax.optimization_barrier((total_two, *joints))
    (own_mixed,) = call_kernel(
        place_kernel,
        [((quarter, 4 * channels), low)],
        [],
        joints,
        "v" * canvas_size,
        1,
        12,
    )
    own_mixed, send_one, send_two = lax.optimization_barrier((own_mixed, send_one, send_two))
    chip_mixed = send_height(own_mixed, 2)
    core_mixed = send_height(own_mixed, 1)
    got_one, got_two = send_phase(send_one, 0), send_phase(send_two, 0)
    own_total, sums, partial_sums = call_kernel(
        functools.partial(first_kernel, cols=cols),
        [((own_pixels, channels), wide), sums_shape, sums_shape],
        [held_wide, taps],
        [total_two, scales, middle, all_features, table, mask, sums, turned],
        "vvvvvvvv",
        1,
        20,
    )
    got_sums, own_sums = send_phase(sums, 0), sums
    sums, core_mixed, got_one, got_two = lax.optimization_barrier(
        (sums, core_mixed, got_one, got_two)
    )
    share_rows = 9 * out_share
    hold_one, send_share, hold_two = call_kernel(
        halve_both_kernel,
        [
            ((share_rows, ci_share), wide),
            ((2 * share_rows, ci_share), low),
            ((share_rows, ci_share), wide),
        ],
        [],
        [keep_one, got_one, keep_two, got_two],
        "vvvv",
        1,
        12,
    )
    got_share = send_phase(send_share, 1)

    def widened(count, rows):
        return [
            pltpu.VMEM((count, rows, 3 * channels), wide),
            pltpu.VMEM((count, rows, channels), wide),
            sem((count, 2)),
        ]

    grad_shapes = [(qkv_weight.shape, wide), (proj_weight.shape, wide)]
    core_mixed, hold_one = lax.optimization_barrier((core_mixed, hold_one))
    qkv_grad, proj_grad = call_kernel(
        join_kernel,
        grad_shapes,
        widened(2, quarter),
        [own_mixed, core_mixed],
        "vv",
        1,
        12,
        "hh",
    )
    qkv_grad, chip_mixed, got_sums = lax.optimization_barrier((qkv_grad, chip_mixed, got_sums))
    sums = own_sums + got_sums
    got_sums = send_phase(sums, 1)
    chip_halves = call_kernel(
        cut_kernel,
        [((quarter // 2, 4 * channels), low)] * 2,
        [],
        [chip_mixed],
        "v",
        1,
        12,
    )
    both_halves = [send_height(half, 1) for half in chip_halves]
    qkv_grad, proj_grad = call_kernel(
        last_kernel,
        grad_shapes,
        widened(4, quarter // 2),
        [chip_mixed, *both_halves, qkv_grad, proj_grad],
        "vvvhh",
        1,
        12,
        "hh",
        {3: 0, 4: 1},
    )
    qkv_grad, own_total = lax.optimization_barrier((qkv_grad, own_total))
    (input_grad,) = call_kernel(
        own_kernel,
        [((own_pixels, channels), low)],
        [],
        [
            own_total,
            partial_sums,
            all_features,
            all_grad,
            total_three,
            residual,
            scales_three,
            table,
        ],
        "v" * 8,
        dot_flops // 4,
        12,
        "o",
    )
    input_grad, got_share, got_sums = lax.optimization_barrier((input_grad, got_share, got_sums))
    vector_shapes = [norm_gains.shape, norm_shifts.shape, conv_biases.shape, qv_bias.shape]
    conv_grad, gains_grad, shifts_grad, biases_grad, qv_grad, proj_bias_grad = call_kernel(
        sums_kernel,
        [((2, 3, 3, out_share, ci_share), wide)]
        + [(shape, wide) for shape in vector_shapes + [(1, channels)]],
        [],
        [sums, got_sums, hold_one, hold_two, got_share],
        "vvvvv",
        1,
        12,
        "o" * 6,
    )
    own_shape = (1, local_rows, cols, channels)
    return (
        output.reshape(own_shape),
        input_grad.reshape(own_shape),
        gains_grad,
        shifts_grad,
        jnp.swapaxes(conv_grad, 3, 4),
        biases_grad,
        qkv_grad,
        qv_grad,
        proj_grad,
        proj_bias_grad.reshape(channels),
    )


def on_device(*arrays):
    features, tile_ids = arrays[0], arrays[1]
    local_rows, cols, channels = features.shape[1:]
    pixels = tile_ids.shape[1] * cols
    height_size, canvas_size = lax.axis_size("height"), lax.axis_size("canvas")
    powers = all(size & (size - 1) == 0 for size in (height_size, canvas_size, cols))
    fits = (
        powers
        and height_size > 2
        and canvas_size == 4
        and channels == LANES * canvas_size
        and pixels <= MOST_PIXELS
        and pixels % FILL_ROWS == 0
        and pixels >= EARLY_ROWS
        and FILL_ROWS % CHUNK == 0
        and pixels % SCORE_ROWS == 0
        and pixels % KEY_ROWS == 0
        and (local_rows * cols) % LANES == 0
        and CHUNK % cols == 0
        and cols % 16 == 0
        and channels % (LANES * canvas_size) == 0
        and 2 * channels == NARROW * height_size
    )
    return whole_canvas(*arrays) if fits else split_canvas(*arrays)


def solution(mesh):
    in_specs = (
        P("canvas", "height", None, None),
        P("canvas", None),
        P(),
        P(),
        P(),
        P(),
        P(),
        P(),
        P(),
        P(),
        P("canvas", "height", None, None),
    )
    out_specs = (
        P("canvas", "height", None, None),
        P("canvas", "height", None, None),
        P(),
        P(),
        P(None, None, None, "canvas", "height"),
        P(),
        P(),
        P(),
        P(),
        P(),
    )
    return jax.shard_map(
        on_device, mesh=mesh, in_specs=in_specs, out_specs=out_specs, check_vma=False
    )
```
